32 devices in a mesh: section: 4 (over y, x), seq: 2 (over core), tensor: 4 (over z).
Axes of the slice: x: 2, y: 2, z: 4, core: 2. Of those that a mesh axis runs over, the one named last changes fastest.
Arguments:
- inputs: bfloat16 [2, 256, 2, 768], P(None, ('seq', 'tensor')), may hold values from -6 to 6
- cotangent: bfloat16 [2, 256, 2, 768], P(None, ('seq', 'tensor')), may hold values from -6 to 6
- lengths: int32 [2, 2], replicated, may hold values from 64 to 256, as said below
- chosen: int32 [4, 2, 2, 12, 4, 64], P('section', None, None, 'tensor', 'seq'), may hold values from 0 to 128, as said below
- ln1_gain: float32 [4, 768], P('section'), may hold values from 0.5 to 1.5
- ln1_shift: float32 [4, 768], P('section'), may hold values from -1.5 to 1.5
- w_qkv: bfloat16 [4, 3, 768, 768], P('section', None, None, 'tensor'), may hold values from -0.21875 to 0.21875
- b_qv: float32 [4, 2, 768], P('section', None, 'tensor'), may hold values from -1.5 to 1.5
- w_out: bfloat16 [4, 768, 768], P('section', 'tensor'), may hold values from -0.625 to 0.625
- b_out: float32 [4, 768], P('section'), may hold values from -1.5 to 1.5
- ln2_gain: float32 [4, 768], P('section'), may hold values from 0.5 to 1.5
- ln2_shift: float32 [4, 768], P('section'), may hold values from -1.5 to 1.5
- w_fc: bfloat16 [4, 768, 3072], P('section', None, 'tensor'), may hold values from -0.21875 to 0.21875
- b_fc: float32 [4, 3072], P('section', 'tensor'), may hold values from -1.5 to 1.5
- w_proj: bfloat16 [4, 3072, 768], P('section', 'tensor'), may hold values from -0.109375 to 0.109375
- b_proj: float32 [4, 768], P('section'), may hold values from -1.5 to 1.5
Outputs:
- activations: bfloat16 [4, 2, 256, 2, 768], P('section', None, ('seq', 'tensor'))
- in_grads: bfloat16 [4, 2, 256, 2, 768], P('section', None, ('seq', 'tensor'))
- grad_ln1_gain: float32 [4, 768], P('section')
- grad_ln1_shift: float32 [4, 768], P('section')
- grad_w_qkv: float32 [4, 3, 768, 768], P('section', None, 'seq', 'tensor')
- grad_b_qv: float32 [4, 2, 768], P('section')
- grad_w_out: float32 [4, 768, 768], P('section', 'tensor', 'seq')
- grad_b_out: float32 [4, 768], P('section')
- grad_ln2_gain: float32 [4, 768], P('section')
- grad_ln2_shift: float32 [4, 768], P('section')
- grad_w_fc: float32 [4, 768, 3072], P('section', 'seq', 'tensor')
- grad_b_fc: float32 [4, 3072], P('section')
- grad_w_proj: float32 [4, 3072, 768], P('section', 'tensor', 'seq')
- grad_b_proj: float32 [4, 768], P('section')
The draws below stay inside these ranges and needn't reach their ends.
Inputs may be any that keep to these rules, and one draw needn't show every extreme that they name: `lengths`: in each micro-batch one sequence, drawn from the seed, is full (256 positions). `chosen`: entries of query block b are positions of the same sequence; where b * 64 >= 64 they lie in 0 to b * 64 - 64 and the last entry of each block and head equals b * 64 - 64; in earlier blocks every entry is 0.
All inputs are finite; a program needn't handle non-finite values.
Results may differ from the reference program's by a relative error of at most 0.025.
Values may be sent and summed in bfloat16 or wider, within the bound.
A program may use at most 192 MiB of HBM per device.

```python
import math
import jax
import jax.numpy as jnp
from jax import lax

D = 768
HEADS = 12
HDIM = 64
FF = 3072
WIN = 64
QB = 64
KSEL = 64
MICRO = 2
NBUCK = 2
SECTIONS = 4
SEQLEN = 256
NQB = 4


def draw_lengths(key, part):
    key = jax.random.fold_in(key, 11)
    ragged_key, slot_key = jax.random.split(key)
    ragged = jax.random.randint(ragged_key, (MICRO, NBUCK), SEQLEN // 4, SEQLEN + 1)
    full_slot = jax.random.randint(slot_key, (MICRO, 1), 0, NBUCK)
    slot_index = lax.broadcasted_iota(jnp.int32, (MICRO, NBUCK), 1)
    return jnp.where(slot_index == full_slot, SEQLEN, ragged).astype(jnp.int32)


def draw_chosen(key, part):
    key = jax.random.fold_in(key, 23)
    shape_full = (SECTIONS, MICRO, NBUCK, HEADS, NQB, KSEL)
    block_start = lax.broadcasted_iota(jnp.int32, shape_full, 4) * QB
    upper_bound = jnp.maximum(block_start - WIN + 1, 1)
    drawn_index = jax.random.randint(key, shape_full, 0, upper_bound)
    last_slot = lax.broadcasted_iota(jnp.int32, shape_full, 5) == KSEL - 1
    return jnp.where(last_slot, upper_bound - 1, drawn_index).astype(jnp.int32)


def block_scale(key, extent, shards, low, top_value):
    def one(axis_at, parts):
        heights = jax.random.uniform(jax.random.fold_in(jax.random.fold_in(key, 6), axis_at), (parts,), jnp.float32, low / len(shards), top_value / len(shards))
        return jnp.repeat(jnp.exp(heights), extent[axis_at] // parts).reshape((-1,) + (1,) * (len(extent) - axis_at - 1))

    level = one(*shards[0])
    for cut in shards[1:]:
        level = level * one(*cut)
    return level


def normal_values(own_key, extent, spread, reach, cuts=(), kind=jnp.bfloat16):
    level = block_scale(own_key, extent, cuts, -0.22, 0.18) if cuts else 1.0
    array = jax.random.normal(own_key, extent, jnp.float32) * spread * level
    return jnp.minimum(jnp.maximum(array, -reach), reach).astype(kind)


def setup_inputs(seed: int = 0) -> dict:
    arg_keys = jax.random.split(jax.random.key(seed), 17)
    inputs = normal_values(arg_keys[0], (MICRO, SEQLEN, NBUCK, D), 1.0, 6.0, ((1, 8),))
    cotangent = normal_values(arg_keys[1], (MICRO, SEQLEN, NBUCK, D), 1.0, 6.0, ((1, 8),))
    lengths = draw_lengths(jax.random.fold_in(arg_keys[16], 71), 0)
    chosen = draw_chosen(jax.random.fold_in(arg_keys[16], 71), 0)
    ln1_gain = jnp.clip(1.0 + 0.1 * jax.random.normal(arg_keys[4], (SECTIONS, D), jnp.float32), 0.5, 1.5)
    ln1_shift = normal_values(arg_keys[5], (SECTIONS, D), 0.3, 1.5, ((0, 4),), jnp.float32)
    w_qkv = normal_values(arg_keys[6], (SECTIONS, 3, D, D), D ** -0.5, 0.21875, ((0, 4), (3, 4)))
    b_qv = normal_values(arg_keys[7], (SECTIONS, 2, D), 0.3, 1.5, ((0, 4), (2, 4)), jnp.float32)
    w_out = normal_values(arg_keys[8], (SECTIONS, D, D), (D // 8) ** -0.5, 0.625, ((0, 4), (1, 4)))
    b_out = normal_values(arg_keys[9], (SECTIONS, D), 0.3, 1.5, ((0, 4),), jnp.float32)
    ln2_gain = jnp.clip(1.0 + 0.1 * jax.random.normal(arg_keys[10], (SECTIONS, D), jnp.float32), 0.5, 1.5)
    ln2_shift = normal_values(arg_keys[11], (SECTIONS, D), 0.3, 1.5, ((0, 4),), jnp.float32)
    w_fc = normal_values(arg_keys[12], (SECTIONS, D, FF), D ** -0.5, 0.21875, ((0, 4), (2, 4)))
    b_fc = normal_values(arg_keys[13], (SECTIONS, FF), 0.3, 1.5, ((0, 4), (1, 4)), jnp.float32)
    w_proj = normal_values(arg_keys[14], (SECTIONS, FF, D), FF ** -0.5, 0.109375, ((0, 4), (1, 4)))
    b_proj = normal_values(arg_keys[15], (SECTIONS, D), 0.3, 1.5, ((0, 4),), jnp.float32)
    return dict(inputs=inputs, cotangent=cotangent, lengths=lengths, chosen=chosen, ln1_gain=ln1_gain, ln1_shift=ln1_shift, w_qkv=w_qkv, b_qv=b_qv, w_out=w_out, b_out=b_out, ln2_gain=ln2_gain, ln2_shift=ln2_shift, w_fc=w_fc, b_fc=b_fc, w_proj=w_proj, b_proj=b_proj)


@jax.custom_vjp
def low(v):
    return lax.optimization_barrier(v.astype(jnp.bfloat16)).astype(jnp.float32)

@jax.custom_vjp
def low_back(v):
    return v

def low_keep(v):
    return (low(v), None)

def low_pass(kept, grad):
    return (grad,)

def back_keep(v):
    return (v, None)

def back_low(kept, grad):
    return (low(grad),)
low.defvjp(low_keep, low_pass)
low_back.defvjp(back_keep, back_low)
NORM_EPS = 1e-05
MASKED = -1000000000.0
HIGHEST = lax.Precision.HIGHEST

def matmul(left_rows, right_rows):
    return jnp.matmul(left_rows, right_rows, precision=HIGHEST)

def layer_norm(values, gain, shift):
    average = lax.optimization_barrier(jnp.mean(values, axis=-1, keepdims=True))
    centred = values - average
    variance = lax.optimization_barrier(jnp.mean(centred * centred, axis=-1, keepdims=True))
    return centred * lax.rsqrt(variance + NORM_EPS) * gain + shift

def gelu_tanh(values):
    return 0.5 * values * (1.0 + jnp.tanh(0.7978845608028654 * (values + 0.044715 * values * values * values)))

def sparse_attention(queries, key_rows, value_rows, chosen):
    score_scale = HDIM ** (-0.5)
    group_size = math.gcd(NQB, max(1, 512 // QB))
    group_count = NQB // group_size
    span = WIN + QB
    query_groups = queries.reshape(group_count, group_size, QB, NBUCK, HEADS, HDIM)
    zero_rows = jnp.zeros_like(key_rows[:WIN])
    padded_keys = jnp.concatenate([zero_rows, key_rows], 0)
    padded_values = jnp.concatenate([zero_rows, value_rows], 0)
    flat_keys = key_rows.reshape(SEQLEN * NBUCK * HEADS, HDIM)
    flat_values = value_rows.reshape(SEQLEN * NBUCK * HEADS, HDIM)
    bucket_ids = lax.broadcasted_iota(jnp.int32, chosen.shape, 0)
    head_ids = lax.broadcasted_iota(jnp.int32, chosen.shape, 1)
    flat_index = (chosen * NBUCK + bucket_ids) * HEADS + head_ids
    index_groups = jnp.moveaxis(flat_index.reshape(NBUCK, HEADS, group_count, group_size, KSEL), 2, 0)
    chosen_groups = jnp.moveaxis(chosen.reshape(NBUCK, HEADS, group_count, group_size, KSEL), 2, 0)
    group_ids = jnp.arange(group_count, dtype=jnp.int32)

    def one_group(pieces):
        query_block, chosen_block, index_block, group_index = pieces
        first_row = group_index * (group_size * QB)

        def slabs(padded):
            segment = lax.dynamic_slice_in_dim(padded, first_row, group_size * QB + WIN, 0)
            segment = segment.reshape(group_size * QB + WIN, NBUCK, HEADS, HDIM)
            return jnp.concatenate([segment[offset_index * QB:offset_index * QB + group_size * QB].reshape(group_size, QB, NBUCK, HEADS, HDIM) for offset_index in range(WIN // QB + 1)], 1)
        near_keys = slabs(padded_keys)
        near_values = slabs(padded_values)
        far_keys = jnp.take(flat_keys, index_block, axis=0)
        far_values = jnp.take(flat_values, index_block, axis=0)
        near_scores = jnp.einsum('bqnhe,btnhe->bnhqt', query_block, near_keys, precision=HIGHEST)
        far_scores = jnp.einsum('bqnhe,nhbke->bnhqk', query_block, far_keys, precision=HIGHEST)
        scores = low_back(score_scale * jnp.concatenate([near_scores, far_scores], -1))
        block_start = first_row + QB * lax.broadcasted_iota(jnp.int32, (group_size, 1, 1), 0)
        query_ids = lax.broadcasted_iota(jnp.int32, (1, QB, 1), 1)
        key_ids = lax.broadcasted_iota(jnp.int32, (1, 1, span), 2)
        distance = query_ids + WIN - key_ids
        near_ok = (distance >= 0) & (distance < WIN) & (block_start + key_ids - WIN >= 0)
        far_ok = chosen_block + WIN <= block_start.reshape(1, 1, group_size, 1)
        near_mask = jnp.broadcast_to(near_ok[:, None, None], (group_size, NBUCK, HEADS, QB, span))
        far_mask = jnp.broadcast_to(jnp.transpose(far_ok, (2, 0, 1, 3))[:, :, :, None, :], (group_size, NBUCK, HEADS, QB, KSEL))
        key_mask = jnp.concatenate([near_mask, far_mask], -1)
        masked = jnp.where(key_mask, scores, MASKED)
        row_top = lax.optimization_barrier(jnp.max(masked, -1, keepdims=True))
        exp_terms = jnp.exp(masked - row_top)
        softmax_low = low(exp_terms / lax.optimization_barrier(jnp.sum(exp_terms, -1, keepdims=True)))
        near_part = jnp.einsum('bnhqt,btnhe->bqnhe', softmax_low[..., :span], near_values, precision=HIGHEST)
        far_part = jnp.einsum('bnhqk,nhbke->bqnhe', softmax_low[..., span:], far_values, precision=HIGHEST)
        return near_part + far_part
    attended = lax.map(jax.checkpoint(one_group), (query_groups, chosen_groups, index_groups, group_ids))
    return attended.reshape(SEQLEN, NBUCK, D)

def residual_block(hidden, section_weights, chosen_now, row_mask):
    ln1_gain, ln1_shift, w_qkv, b_qv, w_out, b_out, ln2_gain, ln2_shift, w_fc, b_fc, w_proj, b_proj = section_weights
    hidden = low_back(hidden)
    normed = low(layer_norm(hidden, ln1_gain, ln1_shift))
    queries = low(low_back(matmul(normed, w_qkv[0]) + b_qv[0]))
    key_rows = low(low_back(matmul(normed, w_qkv[1])))
    value_rows = low(low_back(matmul(normed, w_qkv[2]) + b_qv[1]))
    mixed_rows = sparse_attention(queries, key_rows, value_rows, chosen_now) * row_mask[:, :, None]
    mixed_rows = low(low_back(mixed_rows))
    middle = hidden + low_back(matmul(mixed_rows, w_out) + b_out)
    normed_mlp = low(layer_norm(middle, ln2_gain, ln2_shift))
    pre_active = low_back(matmul(normed_mlp, w_fc) + b_fc)
    active = low(gelu_tanh(pre_active))
    return low(middle + matmul(active, w_proj) + b_proj)

def forward(inputs, offsets, weights, chosen, row_mask):
    outputs = []
    for micro_index in range(MICRO):
        hidden = inputs[micro_index]
        per_section = []
        for section_index in range(SECTIONS):
            section_weights = tuple((weight_array[section_index] for weight_array in weights))
            hidden = residual_block(hidden + offsets[section_index, micro_index], section_weights, chosen[section_index, micro_index], row_mask[micro_index])
            per_section.append(hidden)
        outputs.append(jnp.stack(per_section))
    return jnp.stack(outputs, axis=1)

def reference(inputs, cotangent, lengths, chosen, ln1_gain, ln1_shift, w_qkv, b_qv, w_out, b_out, ln2_gain, ln2_shift, w_fc, b_fc, w_proj, b_proj):
    weights = tuple((weight_array.astype(jnp.float32) for weight_array in (ln1_gain, ln1_shift, w_qkv, b_qv, w_out, b_out, ln2_gain, ln2_shift, w_fc, b_fc, w_proj, b_proj)))
    positions = lax.broadcasted_iota(jnp.int32, (MICRO, SEQLEN, NBUCK), 1)
    row_mask = (positions < lengths[:, None, :]).astype(jnp.float32)
    inputs_wide = inputs.astype(jnp.float32)
    offsets = jnp.zeros((SECTIONS, MICRO, SEQLEN, NBUCK, D), jnp.float32)

    def run_all(offsets_in, weights_in):
        return forward(inputs_wide, offsets_in, weights_in, chosen, row_mask)
    activations, pullback = jax.vjp(run_all, offsets, weights)
    top_grad = jnp.zeros_like(activations).at[SECTIONS - 1].set(cotangent.astype(jnp.float32) * row_mask[..., None])
    grad_offsets, grad_weights = pullback(top_grad)
    return (activations.astype(jnp.bfloat16), grad_offsets.astype(jnp.bfloat16), grad_weights[0], grad_weights[1], grad_weights[2], grad_weights[3], grad_weights[4], grad_weights[5], grad_weights[6], grad_weights[7], grad_weights[8], grad_weights[9], grad_weights[10], grad_weights[11])
```

```python
import functools
import types

import jax
import jax.numpy as jnp
from jax import lax
from jax.experimental import pallas as pl
from jax.experimental.pallas import tpu as pltpu
from jax.sharding import PartitionSpec as P

HDIM = 64
WIN = 64
QB = 64
KSEL = 64


NORM_EPS = 1e-05
MASKED = -1000000000.0


def from_behind(value, axis, steps):
    count = lax.axis_size(axis)
    first, last = (max(0, -steps), min(count, count - steps))
    return lax.ppermute(value, axis, [(source, source + steps) for source in range(first, last)])


def layer_norm(values, gain, shift):
    average = jnp.mean(values, axis=-1, keepdims=True)
    centred = values - average
    variance = jnp.mean(centred * centred, axis=-1, keepdims=True)
    return centred * lax.rsqrt(variance + NORM_EPS) * gain + shift


def gelu_tanh(values):
    return (
        0.5
        * values
        * (1.0 + jnp.tanh(0.7978845608028654 * (values + 0.044715 * values * values * values)))
    )


def gather_rows(row_block):
    return lax.all_gather(row_block, "tensor", axis=0, tiled=True)


def scatter_product(left_rows, weight, formula):
    return lax.psum_scatter(
        jnp.einsum(formula, left_rows, weight, preferred_element_type=jnp.float32).astype(
            jnp.bfloat16
        ),
        "tensor",
        scatter_dimension=0,
        tiled=True,
    ).astype(jnp.float32)


def near_slabs(full_rows, seq_start, seq_first, length_local):
    buckets = full_rows.shape[1]
    heads_local = full_rows.shape[2] // HDIM
    blocks = length_local // QB
    earlier = lax.dynamic_slice_in_dim(full_rows, jnp.maximum(seq_start - WIN, 0), WIN, 0)
    earlier = jnp.where(seq_first, jnp.zeros_like(earlier), earlier)
    local_part = lax.dynamic_slice_in_dim(full_rows, seq_start, length_local, 0)
    segment = jnp.concatenate([earlier, local_part], 0).reshape(
        length_local + WIN, buckets, heads_local, HDIM
    )
    return jnp.concatenate(
        [
            segment[offset_index * QB : offset_index * QB + length_local].reshape(
                blocks, QB, buckets, heads_local, HDIM
            )
            for offset_index in range(WIN // QB + 1)
        ],
        1,
    )


def far_rows(full_rows, flat_index):
    total_rows, buckets, feature_width = full_rows.shape
    heads_local = feature_width // HDIM
    return jnp.take(full_rows.reshape(total_rows * buckets * heads_local, HDIM), flat_index, axis=0)


def key_geometry(chosen_now, seq_start, blocks):
    buckets, heads_local = (chosen_now.shape[0], chosen_now.shape[1])
    bucket_ids = lax.broadcasted_iota(jnp.int32, chosen_now.shape, 0)
    head_ids = lax.broadcasted_iota(jnp.int32, chosen_now.shape, 1)
    flat_index = (chosen_now * buckets + bucket_ids) * heads_local + head_ids
    block_start = seq_start + QB * lax.broadcasted_iota(jnp.int32, (blocks, 1, 1), 0)
    query_ids = lax.broadcasted_iota(jnp.int32, (1, QB, 1), 1)
    key_ids = lax.broadcasted_iota(jnp.int32, (1, 1, WIN + QB), 2)
    distance = query_ids + WIN - key_ids
    near_ok = (distance >= 0) & (distance < WIN) & (block_start + key_ids - WIN >= 0)
    far_ok = chosen_now + WIN <= block_start.reshape(1, 1, blocks, 1)
    near_mask = jnp.broadcast_to(
        near_ok[:, None, None], (blocks, buckets, heads_local, QB, WIN + QB)
    )
    far_mask = jnp.broadcast_to(
        jnp.transpose(far_ok, (2, 0, 1, 3))[:, :, :, None, :],
        (blocks, buckets, heads_local, QB, KSEL),
    )
    return (flat_index, jnp.concatenate([near_mask, far_mask], -1))


def attention_setup(queries, key_rows, value_rows, chosen_now, seq_start, seq_first):
    length_local, buckets, feature_width = queries.shape
    heads_local = feature_width // HDIM
    blocks = length_local // QB
    query_blocks = queries.reshape(blocks, QB, buckets, heads_local, HDIM)
    flat_index, key_mask = key_geometry(chosen_now, seq_start, blocks)
    near_keys = near_slabs(key_rows, seq_start, seq_first, length_local)
    near_values = near_slabs(value_rows, seq_start, seq_first, length_local)
    far_keys = far_rows(key_rows, flat_index)
    far_values = far_rows(value_rows, flat_index)
    near_scores = jnp.einsum(
        "bqnhe,btnhe->bnhqt", query_blocks, near_keys, preferred_element_type=jnp.float32
    )
    far_scores = jnp.einsum(
        "bqnhe,nhbke->bnhqk", query_blocks, far_keys, preferred_element_type=jnp.float32
    )
    scores = jnp.where(
        key_mask, HDIM ** (-0.5) * jnp.concatenate([near_scores, far_scores], -1), MASKED
    )
    return (query_blocks, near_keys, near_values, far_keys, far_values, flat_index, scores)


def attend(queries, key_rows, value_rows, chosen_now, seq_start, seq_first):
    query_blocks, near_keys, near_values, far_keys, far_values, flat_index, scores = (
        attention_setup(queries, key_rows, value_rows, chosen_now, seq_start, seq_first)
    )
    span = WIN + QB
    row_top = jnp.max(scores, -1, keepdims=True)
    exp_terms = jnp.exp(scores - row_top)
    row_total = jnp.sum(exp_terms, -1, keepdims=True)
    softmax_low = (exp_terms / row_total).astype(jnp.bfloat16)
    near_part = jnp.einsum(
        "bnhqt,btnhe->bqnhe",
        softmax_low[..., :span],
        near_values,
        preferred_element_type=jnp.float32,
    )
    far_part = jnp.einsum(
        "bnhqk,nhbke->bqnhe",
        softmax_low[..., span:],
        far_values,
        preferred_element_type=jnp.float32,
    )
    return ((near_part + far_part).reshape(queries.shape), row_top + jnp.log(row_total))


def spread_back(near_grad, far_grad, flat_index, seq_start, seq_first, total_rows):
    blocks, span, buckets, heads_local, head_size = near_grad.shape
    length_local = blocks * QB
    feature_width = heads_local * head_size
    segment = jnp.zeros((length_local + WIN, buckets, heads_local, head_size), jnp.float32)
    for offset_index in range(WIN // QB + 1):
        piece = near_grad[:, offset_index * QB : (offset_index + 1) * QB].reshape(
            length_local, buckets, heads_local, head_size
        )
        segment = segment.at[offset_index * QB : offset_index * QB + length_local].add(piece)
    full_rows = jnp.zeros((total_rows * buckets * heads_local, head_size), jnp.float32)
    full_rows = full_rows.at[flat_index.reshape(-1)].add(far_grad.reshape(-1, head_size))
    full_rows = full_rows.reshape(total_rows, buckets, feature_width)
    local_part = segment[WIN:].reshape(length_local, buckets, feature_width)
    earlier = jnp.where(seq_first, 0.0, segment[:WIN].reshape(WIN, buckets, feature_width))
    full_rows = lax.dynamic_update_slice_in_dim(
        full_rows,
        lax.dynamic_slice_in_dim(full_rows, seq_start, length_local, 0) + local_part,
        seq_start,
        0,
    )
    earlier_start = jnp.maximum(seq_start - WIN, 0)
    full_rows = lax.dynamic_update_slice_in_dim(
        full_rows,
        lax.dynamic_slice_in_dim(full_rows, earlier_start, WIN, 0) + earlier,
        earlier_start,
        0,
    )
    return full_rows


def attend_back(
    queries, key_rows, value_rows, chosen_now, seq_start, seq_first, log_total, grad_mixed
):
    query_blocks, near_keys, near_values, far_keys, far_values, flat_index, scores = (
        attention_setup(queries, key_rows, value_rows, chosen_now, seq_start, seq_first)
    )
    span = WIN + QB
    score_scale = HDIM ** (-0.5)
    grad_blocks = grad_mixed.reshape(query_blocks.shape)
    weights_full = jnp.exp(scores - log_total)
    softmax_low = weights_full.astype(jnp.bfloat16)
    grad_near_weights = jnp.einsum(
        "bqnhe,btnhe->bnhqt", grad_blocks, near_values, preferred_element_type=jnp.float32
    )
    grad_far_weights = jnp.einsum(
        "bqnhe,nhbke->bnhqk", grad_blocks, far_values, preferred_element_type=jnp.float32
    )
    grad_weights = jnp.concatenate([grad_near_weights, grad_far_weights], -1)
    row_dot = jnp.sum(weights_full * grad_weights, -1, keepdims=True)
    grad_scores = (weights_full * (grad_weights - row_dot)).astype(jnp.bfloat16)
    grad_near, grad_far = (grad_scores[..., :span], grad_scores[..., span:])
    grad_queries = score_scale * (
        jnp.einsum("bnhqt,btnhe->bqnhe", grad_near, near_keys, preferred_element_type=jnp.float32)
        + jnp.einsum("bnhqk,nhbke->bqnhe", grad_far, far_keys, preferred_element_type=jnp.float32)
    )
    near_key_grad = score_scale * jnp.einsum(
        "bnhqt,bqnhe->btnhe", grad_near, query_blocks, preferred_element_type=jnp.float32
    )
    far_key_grad = score_scale * jnp.einsum(
        "bnhqk,bqnhe->nhbke", grad_far, query_blocks, preferred_element_type=jnp.float32
    )
    near_value_grad = jnp.einsum(
        "bnhqt,bqnhe->btnhe",
        softmax_low[..., :span],
        grad_blocks,
        preferred_element_type=jnp.float32,
    )
    far_value_grad = jnp.einsum(
        "bnhqk,bqnhe->nhbke",
        softmax_low[..., span:],
        grad_blocks,
        preferred_element_type=jnp.float32,
    )
    total_rows = key_rows.shape[0]
    key_grad = spread_back(
        near_key_grad, far_key_grad, flat_index, seq_start, seq_first, total_rows
    )
    value_grad = spread_back(
        near_value_grad, far_value_grad, flat_index, seq_start, seq_first, total_rows
    )
    return (grad_queries.reshape(queries.shape), key_grad, value_grad)


def forward_pass(hidden, params, chosen_now, query_mask, seq_start, seq_first, finish):
    (
        ln1_gain,
        ln1_shift,
        w_qkv,
        b_qv,
        w_out,
        b_out,
        ln2_gain,
        ln2_shift,
        w_fc,
        b_fc,
        w_proj,
        b_proj,
    ) = params
    hidden_wide = hidden.astype(jnp.float32)
    normed_all = gather_rows(layer_norm(hidden_wide, ln1_gain, ln1_shift).astype(jnp.bfloat16))
    projected = jnp.einsum("pnd,jdc->jpnc", normed_all, w_qkv, preferred_element_type=jnp.float32)
    queries = (projected[0] + b_qv[0]).astype(jnp.bfloat16)
    key_rows, value_rows = (
        lax.all_gather(projected[1].astype(jnp.bfloat16), "seq", axis=0, tiled=True),
        lax.all_gather((projected[2] + b_qv[1]).astype(jnp.bfloat16), "seq", axis=0, tiled=True),
    )
    attended, log_total = attend(queries, key_rows, value_rows, chosen_now, seq_start, seq_first)
    mixed_rows = (attended * query_mask[:, :, None]).astype(jnp.bfloat16)
    middle = hidden_wide + scatter_product(mixed_rows, w_out, "pnc,cd->pnd") + b_out
    normed_mlp = gather_rows(layer_norm(middle, ln2_gain, ln2_shift).astype(jnp.bfloat16))
    pre_active = (
        jnp.einsum("pnd,df->pnf", normed_mlp, w_fc, preferred_element_type=jnp.float32) + b_fc
    )
    active = gelu_tanh(pre_active).astype(jnp.bfloat16)
    if not finish:
        return (
            normed_all,
            queries,
            key_rows,
            value_rows,
            log_total,
            mixed_rows,
            middle,
            normed_mlp,
            pre_active,
            active,
        )
    output = (middle + scatter_product(active, w_proj, "pnf,fd->pnd") + b_proj).astype(jnp.bfloat16)
    return (output, (key_rows, value_rows))


def backward_pass(hidden, upstream, params, chosen_now, query_mask, seq_start, seq_first):
    (
        ln1_gain,
        ln1_shift,
        w_qkv,
        b_qv,
        w_out,
        b_out,
        ln2_gain,
        ln2_shift,
        w_fc,
        b_fc,
        w_proj,
        b_proj,
    ) = params
    (
        normed_all,
        queries,
        key_rows,
        value_rows,
        log_total,
        mixed_rows,
        middle,
        normed_mlp,
        pre_active,
        active,
    ) = forward_pass(hidden, params, chosen_now, query_mask, seq_start, seq_first, False)
    upstream_all = gather_rows(upstream)
    grad_w_proj = jnp.einsum(
        "pnf,pnd->fd", active, upstream_all, preferred_element_type=jnp.float32
    )
    grad_b_proj = jnp.sum(upstream.astype(jnp.float32), axis=(0, 1))
    grad_active = jnp.einsum(
        "pnd,fd->pnf", upstream_all, w_proj, preferred_element_type=jnp.float32
    )
    unused_value, gelu_pull = jax.vjp(gelu_tanh, pre_active)
    grad_pre = gelu_pull(grad_active)[0].astype(jnp.bfloat16)
    grad_w_fc = jnp.einsum("pnd,pnf->df", normed_mlp, grad_pre, preferred_element_type=jnp.float32)
    grad_b_fc = jnp.sum(grad_pre.astype(jnp.float32), axis=(0, 1))
    grad_normed_mlp = scatter_product(grad_pre, w_fc, "pnf,df->pnd")
    unused_norm, second_pull = jax.vjp(layer_norm, middle, ln2_gain, ln2_shift)
    grad_mid_norm, grad_ln2_gain, grad_ln2_shift = second_pull(grad_normed_mlp)
    grad_middle = upstream.astype(jnp.float32) + grad_mid_norm
    grad_branch = grad_middle.astype(jnp.bfloat16)
    grad_b_out = jnp.sum(grad_branch.astype(jnp.float32), axis=(0, 1))
    branch_all = gather_rows(grad_branch)
    grad_w_out = jnp.einsum(
        "pnc,pnd->cd", mixed_rows, branch_all, preferred_element_type=jnp.float32
    )
    grad_mixed = jnp.einsum(
        "pnd,cd->pnc", branch_all, w_out, preferred_element_type=jnp.float32
    ).astype(jnp.bfloat16) * query_mask[:, :, None].astype(jnp.bfloat16)
    grad_queries, key_grad_all, value_grad_all = attend_back(
        queries, key_rows, value_rows, chosen_now, seq_start, seq_first, log_total, grad_mixed
    )
    key_grad, value_grad = (
        lax.psum_scatter(
            key_grad_all.astype(jnp.bfloat16), "seq", scatter_dimension=0, tiled=True
        ).astype(jnp.float32),
        lax.psum_scatter(
            value_grad_all.astype(jnp.bfloat16), "seq", scatter_dimension=0, tiled=True
        ).astype(jnp.float32),
    )
    grad_project = jnp.stack(
        [
            grad_queries.astype(jnp.bfloat16),
            key_grad.astype(jnp.bfloat16),
            value_grad.astype(jnp.bfloat16),
        ],
        2,
    )
    grad_w_qkv = jnp.einsum(
        "pnd,pnjc->jdc", normed_all, grad_project, preferred_element_type=jnp.float32
    )
    grad_b_qv = jnp.sum(grad_project[:, :, 0::2].astype(jnp.float32), axis=(0, 1))
    grad_normed = scatter_product(grad_project, w_qkv, "pnjc,jdc->pnd")
    unused_first, first_pull = jax.vjp(layer_norm, hidden.astype(jnp.float32), ln1_gain, ln1_shift)
    grad_in_norm, grad_ln1_gain, grad_ln1_shift = first_pull(grad_normed)
    grad_hidden = (grad_middle + grad_in_norm).astype(jnp.bfloat16)
    block_grads = (
        grad_ln1_gain,
        grad_ln1_shift,
        grad_w_qkv,
        grad_b_qv,
        grad_w_out,
        grad_b_out,
        grad_ln2_gain,
        grad_ln2_shift,
        grad_w_fc,
        grad_b_fc,
        grad_w_proj,
        grad_b_proj,
    )
    return (grad_hidden, block_grads)


def on_device(
    inputs,
    cotangent,
    lengths,
    chosen,
    ln1_gain,
    ln1_shift,
    w_qkv,
    b_qv,
    w_out,
    b_out,
    ln2_gain,
    ln2_shift,
    w_fc,
    b_fc,
    w_proj,
    b_proj,
):
    params = tuple(
        (
            weight_array[0]
            for weight_array in (
                ln1_gain,
                ln1_shift,
                w_qkv,
                b_qv,
                w_out,
                b_out,
                ln2_gain,
                ln2_shift,
                w_fc,
                b_fc,
                w_proj,
                b_proj,
            )
        )
    )
    section_index = lax.axis_index("section")
    section_count = lax.axis_size("section")
    seq_index = lax.axis_index("seq")
    tensor_index = lax.axis_index("tensor")
    tensor_count = lax.axis_size("tensor")
    micro_count, rows_local, buckets, feature_width = inputs.shape
    length_local = rows_local * tensor_count
    heads_width = w_qkv.shape[-1]
    seq_start = seq_index * length_local
    seq_first = seq_index == 0
    positions = seq_start + lax.broadcasted_iota(jnp.int32, (micro_count, length_local, buckets), 1)
    mask_all = (positions < lengths[:, None, :]).astype(jnp.float32)
    mask_rows = lax.dynamic_slice_in_dim(mask_all, tensor_index * rows_local, rows_local, 1)
    step_count = micro_count + section_count - 1
    chosen_section = chosen[0]
    received = jnp.zeros((rows_local, buckets, feature_width), jnp.bfloat16)
    stored = jnp.zeros((micro_count, rows_local, buckets, feature_width), jnp.bfloat16)
    outputs = jnp.zeros_like(stored)
    for step_index in range(step_count):
        micro_index = step_index - section_index
        running = (micro_index >= 0) & (micro_index < micro_count)
        slot_index = jnp.clip(micro_index, 0, micro_count - 1)
        block_in = jnp.where(
            section_index == 0, lax.dynamic_index_in_dim(inputs, slot_index, 0, False), received
        )
        chosen_now = lax.dynamic_index_in_dim(chosen_section, slot_index, 0, False)
        query_mask = lax.dynamic_index_in_dim(mask_all, slot_index, 0, False)
        result, key_pair = forward_pass(
            block_in, params, chosen_now, query_mask, seq_start, seq_first, True
        )
        stored = jnp.where(
            running, lax.dynamic_update_index_in_dim(stored, block_in, slot_index, 0), stored
        )
        outputs = jnp.where(
            running, lax.dynamic_update_index_in_dim(outputs, result, slot_index, 0), outputs
        )
        received = from_behind(result, "section", 1)
    back_received = jnp.zeros((rows_local, buckets, feature_width), jnp.bfloat16)
    in_grads = jnp.zeros_like(stored)
    totals = None
    for step_index in range(step_count):
        micro_index = step_index - (section_count - 1 - section_index)
        running = (micro_index >= 0) & (micro_index < micro_count)
        slot_index = jnp.clip(micro_index, 0, micro_count - 1)
        chosen_now = lax.dynamic_index_in_dim(chosen_section, slot_index, 0, False)
        query_mask = lax.dynamic_index_in_dim(mask_all, slot_index, 0, False)
        local_mask = lax.dynamic_index_in_dim(mask_rows, slot_index, 0, False)
        top_grad = (
            lax.dynamic_index_in_dim(cotangent, slot_index, 0, False).astype(jnp.float32)
            * local_mask[:, :, None]
        ).astype(jnp.bfloat16)
        upstream = jnp.where(section_index == section_count - 1, top_grad, back_received)
        hidden = lax.dynamic_index_in_dim(stored, slot_index, 0, False)
        grad_hidden, block_grads = backward_pass(
            hidden, upstream, params, chosen_now, query_mask, seq_start, seq_first
        )
        block_grads = tuple(
            (jnp.where(running, grad_part, jnp.zeros_like(grad_part)) for grad_part in block_grads)
        )
        totals = (
            block_grads
            if step_index == 0
            else tuple(
                (total_part + grad_part for total_part, grad_part in zip(totals, block_grads))
            )
        )
        in_grads = jnp.where(
            running, lax.dynamic_update_index_in_dim(in_grads, grad_hidden, slot_index, 0), in_grads
        )
        back_received = from_behind(grad_hidden, "section", -1)
    (
        sum_ln1_gain,
        sum_ln1_shift,
        sum_w_qkv,
        sum_b_qv,
        sum_w_out,
        sum_b_out,
        sum_ln2_gain,
        sum_ln2_shift,
        sum_w_fc,
        sum_b_fc,
        sum_w_proj,
        sum_b_proj,
    ) = totals
    part_qkv, part_out, part_fc, part_proj = (
        lax.psum_scatter(
            sum_w_qkv.astype(jnp.bfloat16), "seq", scatter_dimension=1, tiled=True
        ).astype(jnp.float32),
        lax.psum_scatter(
            sum_w_out.astype(jnp.bfloat16), "seq", scatter_dimension=1, tiled=True
        ).astype(jnp.float32),
        lax.psum_scatter(
            sum_w_fc.astype(jnp.bfloat16), "seq", scatter_dimension=0, tiled=True
        ).astype(jnp.float32),
        lax.psum_scatter(
            sum_w_proj.astype(jnp.bfloat16), "seq", scatter_dimension=1, tiled=True
        ).astype(jnp.float32),
    )
    bias_qv = lax.dynamic_update_slice_in_dim(
        jnp.zeros((2, feature_width), jnp.float32), sum_b_qv, tensor_index * heads_width, 1
    )
    units_local = sum_b_fc.shape[0]
    bias_fc = lax.dynamic_update_slice_in_dim(
        jnp.zeros((units_local * tensor_count,), jnp.float32),
        sum_b_fc,
        tensor_index * units_local,
        0,
    )
    small_sums = lax.psum(
        (
            sum_ln1_gain,
            sum_ln1_shift,
            bias_qv,
            sum_b_out,
            sum_ln2_gain,
            sum_ln2_shift,
            bias_fc,
            sum_b_proj,
        ),
        ("seq", "tensor"),
    )
    return (
        outputs[None],
        in_grads[None],
        small_sums[0][None],
        small_sums[1][None],
        part_qkv[None],
        small_sums[2][None],
        part_out[None],
        small_sums[3][None],
        small_sums[4][None],
        small_sums[5][None],
        part_fc[None],
        small_sums[6][None],
        part_proj[None],
        small_sums[7][None],
    )


STREAMS = 2
NRM, NMLP, UPS, BRN, ACT, GPRE, MIX, DQKV = range(8)
F32 = jnp.float32
LOW = jnp.bfloat16
MESH_ID = pl.DeviceIdType.MESH


def dot_nn(left, right):
    return lax.dot_general(left, right, (((1,), (0,)), ((), ())), preferred_element_type=F32)


def dot_nt(left, right):
    return lax.dot_general(left, right, (((1,), (1,)), ((), ())), preferred_element_type=F32)


def dot_tn(left, right):
    return lax.dot_general(left, right, (((0,), (0,)), ((), ())), preferred_element_type=F32)


def standard(rows):
    centred = rows - jnp.mean(rows, axis=-1, keepdims=True)
    scale = lax.rsqrt(jnp.mean(centred * centred, axis=-1, keepdims=True) + NORM_EPS)
    return centred * scale, scale


def standard_back(grad, xhat, scale):
    inner = jnp.mean(grad * xhat, axis=-1, keepdims=True)
    return scale * (grad - jnp.mean(grad, axis=-1, keepdims=True) - xhat * inner)


def column_sum(rows):
    return jnp.sum(rows.astype(F32), axis=0, keepdims=True)


def relay_kernel(names, *refs):
    r = types.SimpleNamespace(**dict(zip(names, refs)))
    a, c, t = (lax.axis_index(name) for name in ("section", "seq", "tensor"))
    lines = lax.axis_size("section")
    chips = lax.axis_size("tensor")
    rows, buckets, width = r.inputs.shape[1:]
    half_width = width // 2
    local = rows * chips
    total = 2 * local
    sub = rows // STREAMS
    stream_rows = local // STREAMS
    head_width = r.wo_in.shape[0]
    heads = head_width // HDIM
    blocks = local // QB
    units = r.wp_in.shape[0]
    scale = HDIM ** (-0.5)
    streams = range(STREAMS)

    def remote(src, dst, send, recv, **target):
        return pltpu.make_async_remote_copy(
            src_ref=src,
            dst_ref=dst,
            send_sem=send,
            recv_sem=recv,
            device_id=target,
            device_id_type=MESH_ID,
        )

    def drain(ref, sem):
        pltpu.make_async_copy(ref, ref, sem).wait()

    def row_block(index, size):
        return pl.ds(pl.multiple_of(index * size, size), size)

    mine = row_block(t, sub)
    my_half = row_block(c, local)

    barrier = pltpu.get_barrier_semaphore()
    for core in range(2):
        for step in range(1, chips):
            there = {"tensor": (t + step) % chips, "seq": core}
            pl.semaphore_signal(barrier, inc=1, device_id=there, device_id_type=MESH_ID)
        for step in range(1, lines):
            there = {"section": (a + step) % lines, "seq": core}
            pl.semaphore_signal(barrier, inc=1, device_id=there, device_id_type=MESH_ID)
    pl.semaphore_signal(barrier, inc=1, device_id={"seq": 1 - c}, device_id_type=MESH_ID)
    pl.semaphore_wait(barrier, 2 * (chips - 1) + 2 * (lines - 1) + 1)

    def beside(s):
        return s + 1 - 2 * (s % 2)

    def above(s):
        return (s + 2) % 4

    def store(p):
        return (r.wq, r.wo, r.wf, r.wp)[p]

    def source(p):
        return (r.wq_in, r.wo_in, r.wf_in, r.wp_in)[p]

    def height(p):
        return source(p).shape[0]

    def core_half(p, s, core):
        return store(p).at[s, row_block(core, height(p) // 2)]

    def first_hop(p, s, neighbour, which):
        return remote(
            source(p).at[row_block(c, height(p) // 2)],
            core_half(p, s, c),
            r.w_first_s.at[p, which],
            r.w_first_r.at[s, p],
            section=neighbour,
        )

    def second_hop(p, s, which):
        view = store(p).at[s, row_block(2 * c + which, height(p) // 4)]
        return remote(
            view, view, r.w_second_s.at[s, p], r.w_second_r.at[s, p, which], section=3 - s
        )

    def core_hop(p, s, core):
        view = core_half(p, s, core)
        return remote(view, view, r.w_core_s.at[s, p], r.w_core_r.at[s, p], seq=1 - c)

    def own_copy(p):
        return pltpu.make_async_copy(source(p), store(p).at[a], r.w_own.at[p])

    def pass_on(s, p):
        for which, line in enumerate((beside(s), above(s))):

            @pl.when(a == line)
            def _():
                first_hop(p, s, line, which).wait_recv()
                second_hop(p, s, which).start()
                core_hop(p, s, c).start()

    def pass_far(s, p):
        @pl.when(a == 3 - s)
        def _():
            second_hop(p, s, 0).wait_recv()
            second_hop(p, s, 1).wait_recv()
            core_hop(p, s, c).start()

    def need(s, p):
        @pl.when(s == 0)
        def _():
            pass_on(s, p)
            pass_far(s, p)

        @pl.when(a == s)
        def _():
            own_copy(p).wait()

        @pl.when(a != s)
        def _():
            core_hop(p, s, 1 - c).wait_recv()

    def small_copy(step, line, slot):
        return remote(
            r.small_own, r.small.at[slot], r.small_s.at[step], r.small_r.at[slot], section=line
        )

    def count_copy(step, line, slot):
        return remote(
            r.count_own.at[line],
            r.count.at[slot],
            r.count_s.at[step],
            r.count_r.at[slot],
            section=line,
        )

    singles = (r.ln1_gain, r.ln1_shift, r.ln2_gain, r.ln2_shift, r.b_out, r.b_proj)
    for place, single in enumerate(singles):
        r.small_own[place : place + 1] = single[...]
    r.small_own[6:7, :units] = r.b_fc[...]
    r.small_own[7:8, :head_width] = r.b_qv[0:1]
    r.small_own[7:8, half_width : half_width + head_width] = r.b_qv[1:2]
    for step in range(1, lines):
        small_copy(step - 1, (a + step) % lines, a).start()
    for p in range(4):
        for which, line in enumerate((beside(a), above(a))):
            first_hop(p, a, line, which).start()
    for p in range(4):
        own_copy(p).start()
    r.small[a] = r.small_own[...]

    def place_of(index):
        inside = index % local
        stream, left = inside // stream_rows, inside % stream_rows
        return (index // local) * local + (left // sub) * rows + stream * sub + left % sub

    def iota(shape, dimension):
        return lax.broadcasted_iota(jnp.int32, shape, dimension)

    square = jnp.where(iota((KSEL, KSEL), 0) == iota((KSEL, KSEL), 1), 1.0, 0.0).astype(LOW)
    position = place_of(iota((KSEL, total), 1)).astype(F32)
    for pair in range(lines * heads):
        line, head = pair // heads, pair % heads
        columns = dot_nt(square, r.chosen[pair].astype(F32).astype(LOW))
        for block in range(blocks):
            pick = head * blocks + block
            r.count_own[line, pick : pick + 1, :] = jnp.sum(
                jnp.where(columns[:, block : block + 1] == position, 1.0, 0.0),
                axis=0,
                keepdims=True,
            )
    for step in range(1, lines):
        count_copy(step - 1, (a + step) % lines, a).start()
    r.count[a] = r.count_own[a]

    partners = (3 - t, (t + 2) % 4, t + 1 - 2 * (t % 2))

    def gather(buffer, s, kind, j, slot, chip):
        view = buffer.at[s, j, row_block(chip, sub)]
        return remote(
            view,
            view,
            r.ag_s.at[kind, j, slot],
            r.ag_r.at[kind, j, slot],
            tensor=partners[slot],
        )

    def gather_start(buffer, s, kind, j):
        for slot in range(chips - 1):
            gather(buffer, s, kind, j, slot, t).start()

    def gather_wait(buffer, s, kind, j):
        for slot in range(chips - 1):
            gather(buffer, s, kind, j, slot, partners[slot]).wait_recv()
        for slot in range(chips - 1):
            gather(buffer, s, kind, j, slot, t).wait_send()

    def scatter(s, kind, j, slot):
        return remote(
            r.part.at[kind, j, row_block(partners[slot], sub)],
            r.arrived.at[s, kind, j, slot],
            r.rs_s.at[kind, j, slot],
            r.rs_r.at[kind, j, slot],
            tensor=partners[slot],
        )

    def scatter_start(s, kind, j, product):
        r.part[kind, j] = product.astype(LOW)
        for slot in range(chips - 1):
            scatter(s, kind, j, slot).start()

    def scatter_sum(s, kind, j):
        result = r.part[kind, j, mine].astype(F32)
        for slot in range(chips - 1):
            scatter(s, kind, j, slot).wait_recv()
            result = result + r.arrived[s, kind, j, slot].astype(F32)
        for slot in range(chips - 1):
            scatter(s, kind, j, slot).wait_send()
        return result

    own_rows = (r.nrm, r.nmlp, r.ups, r.brn, r.act, r.gpre, r.mix, r.dqkv)
    all_rows = (
        r.all_nrm,
        r.all_nmlp,
        r.all_ups,
        r.all_brn,
        r.all_act,
        r.all_gpre,
        r.all_mix,
        r.all_dqkv,
    )

    def rows_copy(index, s, same, stays=False):
        core = c if same else 1 - c
        src = own_rows[index].at[s]
        dst = all_rows[index].at[a, c]
        if index <= BRN:
            src = src.at[:, :, row_block(core, half_width)]
        recv = r.rows_r.at[index]
        if stays:
            return pltpu.make_async_copy(src, dst, recv)
        if same:
            return remote(src, dst, r.rows_s.at[index, s, 0], recv, section=s)
        return remote(src, dst, r.rows_s.at[index, s, 1], recv, section=s, seq=1 - c)

    def rows_start(index, s):
        @pl.when(a == s)
        def _():
            rows_copy(index, s, True, True).start()

        @pl.when(a != s)
        def _():
            rows_copy(index, s, True).start()

        rows_copy(index, s, False).start()

    def rows_sent(index, s):
        @pl.when(a != s)
        def _():
            rows_copy(index, s, True).wait_send()

        rows_copy(index, s, False).wait_send()

    def home_copy(src, dst, send, recv, s):
        return remote(src.at[s], dst.at[a], send.at[s], recv, section=s)

    def home_start(src, dst, send, recv, s):
        @pl.when(a == s)
        def _():
            pltpu.make_async_copy(src.at[s], dst.at[a], recv).start()

        @pl.when(a != s)
        def _():
            home_copy(src, dst, send, recv, s).start()

    def home_sent(*what):
        @pl.when(a != what[-1])
        def _():
            home_copy(*what).wait_send()

    out_home = (r.out_low, r.acts, r.out_s, r.out_r)
    grad_home = (r.grad_low, r.grads, r.grad_s, r.grad_r)
    norm_home = (r.norm_part, r.norm_all, r.norm_s, r.norm_r)

    length = r.lengths[a // buckets, a % buckets]
    query = place_of(c * local + iota((local, total), 0))
    key = place_of(iota((local, total), 1))
    near = jnp.where((query >= key) & (query - key < WIN), 1.0, 0.0)
    key_row = place_of(iota((1, total), 1))
    block_of = place_of(iota((local, total), 0)) // QB
    first_block = jnp.where(block_of == 0, 1.0, 0.0)

    def row_mask(place):
        return jnp.where(place < length, 1.0, 0.0)

    def multiplicity(s, head):
        times = near
        for block in range(blocks):
            pick = head * blocks + block
            limit = (c * blocks + block) * QB - WIN
            counted = jnp.where(key_row <= limit, r.count[s, pick : pick + 1, :], 0.0)
            times = times + jnp.where(block_of == block, counted, 0.0)
        return times

    def head_cols(head):
        return slice(head * HDIM, (head + 1) * HDIM)

    def kv_copy(s, core):
        view = r.kv.at[s, :, row_block(core, local)]
        return remote(view, view, r.kv_s.at[s], r.kv_r.at[s], seq=1 - c)

    def dkv_copy(s):
        return remote(r.dkv_out.at[s], r.dkv_in.at[s], r.dkv_s.at[s], r.dkv_r.at[s], seq=1 - c)

    def flat(array):
        return array.reshape(local, array.shape[-1])

    def own_sequence(ref):
        both = ref[a // buckets].astype(F32)
        picked = both[:, 0, :]
        for bucket in range(1, buckets):
            picked = jnp.where(a % buckets == bucket, both[:, bucket, :], picked)
        return picked

    def part_rows(j):
        return slice(j * sub, (j + 1) * sub)

    r.hidden[...] = own_sequence(r.inputs)
    own_place = c * local + t * rows + iota((rows, 1), 0)
    r.upstream[...] = (own_sequence(r.cotangent) * row_mask(own_place)).astype(LOW)
    r.norm_part[...] = jnp.zeros_like(r.norm_part)

    def enter(s, j):
        xhat, inverse = standard(r.hidden[part_rows(j)])
        r.xhat1[s, j] = xhat
        r.inv1[s, j] = jnp.broadcast_to(inverse, (sub, 128))
        r.nrm[s, j, mine] = (xhat * r.small[s, 0:1] + r.small[s, 1:2]).astype(LOW)
        gather_start(r.nrm, s, 0, j)

    def project(s, j):
        gather_wait(r.nrm, s, 0, j)
        normed = r.nrm[s, j]
        place = row_block(c * STREAMS + j, stream_rows)
        bias_v = r.small[s, 7:8, half_width : half_width + head_width]
        key_rows = dot_nt(normed, r.wq[s, head_width : 2 * head_width])
        value_rows = dot_nt(normed, r.wq[s, 2 * head_width : 3 * head_width]) + bias_v
        r.kv[s, 0, place] = key_rows.astype(LOW)
        r.kv[s, 1, place] = value_rows.astype(LOW)

    def ask(s, j):
        queries = dot_nt(r.nrm[s, j], r.wq[s, 0:head_width]) + r.small[s, 7:8, :head_width]
        r.qry[s, j] = queries.astype(LOW)

    def attend_line(s):
        mixed = []
        queries = flat(r.qry[s])
        for head in range(heads):
            times = multiplicity(s, head)
            scores = scale * dot_nt(queries[:, head_cols(head)], r.kv[s, 0, :, head_cols(head)])
            scores = jnp.where(times > 0.0, scores, MASKED)
            top = jnp.max(scores, axis=-1, keepdims=True)
            terms = times * jnp.exp(scores - top)
            weights = terms / jnp.sum(terms, axis=-1, keepdims=True)
            r.soft[s, head] = weights
            mixed.append(dot_nn(weights.astype(LOW), r.kv[s, 1, :, head_cols(head)]))
        mask = row_mask(place_of(c * local + iota((local, 1), 0)))
        mixed = (jnp.concatenate(mixed, axis=-1) * mask).astype(LOW)
        r.mix[s] = mixed.reshape(r.mix.shape[1:])

    def leave_attention(s, j):
        scatter_start(s, 0, j, dot_nn(r.mix[s, j], r.wo[s]))

    def between(s, j):
        middle = r.hidden[part_rows(j)] + scatter_sum(s, 0, j) + r.small[s, 4:5]
        r.middle[part_rows(j)] = middle
        xhat, inverse = standard(middle)
        r.xhat2[s, j] = xhat
        r.inv2[s, j] = jnp.broadcast_to(inverse, (sub, 128))
        r.nmlp[s, j, mine] = (xhat * r.small[s, 2:3] + r.small[s, 3:4]).astype(LOW)
        gather_start(r.nmlp, s, 1, j)

    def feed(s, j):
        gather_wait(r.nmlp, s, 1, j)
        before = dot_nn(r.nmlp[s, j], r.wf[s]) + r.small[s, 6:7, :units]
        bend = jnp.tanh(0.7978845608028654 * (before + 0.044715 * before * before * before))
        r.act[s, j] = (0.5 * before * (1.0 + bend)).astype(LOW)
        r.slope[s, j] = 0.5 * (1.0 + bend) + 0.5 * before * (1.0 - bend * bend) * (
            0.7978845608028654 * (1.0 + 3 * 0.044715 * before * before)
        )

    def leave_feed(s, j):
        scatter_start(s, 1, j, dot_nn(r.act[s, j], r.wp[s]))

    def finish(s, j):
        result = r.middle[part_rows(j)] + scatter_sum(s, 1, j) + r.small[s, 5:6]
        r.out_low[s, part_rows(j)] = result.astype(LOW)
        r.hidden[part_rows(j)] = result.astype(LOW).astype(F32)

    def small_ready(s):
        @pl.when(a != s)
        def _():
            small_copy(0, a, s).wait_recv()

    small_ready(0)
    for j in streams:
        enter(0, j)

    def forward(s, _):
        need(s, 0)
        for j in streams:
            project(s, j)
        kv_copy(s, c).start()
        for j in streams:
            ask(s, j)
        rows_start(NRM, s)

        @pl.when(a != s)
        def _():
            count_copy(0, a, s).wait_recv()

        kv_copy(s, 1 - c).wait_recv()
        attend_line(s)
        need(s, 1)
        for j in streams:
            leave_attention(s, j)
        rows_start(MIX, s)
        for j in streams:
            between(s, j)
        need(s, 2)
        for j in streams:
            feed(s, j)
            if j == 0:
                need(s, 3)
            leave_feed(s, j)
        rows_start(NMLP, s)
        rows_start(ACT, s)

        @pl.when(s + 1 < lines)
        def _():
            small_ready(s + 1)

        for j in streams:
            finish(s, j)

            @pl.when(s + 1 < lines)
            def _():
                enter(s + 1, j)

        home_start(*out_home, s)

        @pl.when(s == 0)
        def _():
            for later in range(1, lines):
                for p in range(4):
                    pass_on(later, p)

        @pl.when(s + 1 < lines)
        def _():
            for p in range(4):
                pass_far(s + 1, p)

        return 0

    lax.fori_loop(0, lines, forward, 0)

    def turn(s, j):
        upstream = r.upstream[part_rows(j)]
        r.ups[s, j, mine] = upstream
        gather_start(r.ups, s, 2, j)
        r.norm_part[s, 5:6] += column_sum(upstream)

    def feed_back(s, j):
        gather_wait(r.ups, s, 2, j)
        grad_pre = (dot_nt(r.ups[s, j], r.wp[s]) * r.slope[s, j]).astype(LOW)
        r.gpre[s, j] = grad_pre
        scatter_start(s, 2, j, dot_nt(grad_pre, r.wf[s]))
        r.norm_part[s, 6:7, :units] += column_sum(grad_pre)

    def between_back(s, j):
        grad = scatter_sum(s, 2, j)
        xhat = r.xhat2[s, j]
        upstream = r.upstream[part_rows(j)].astype(F32)
        grad_middle = upstream + standard_back(
            grad * r.small[s, 2:3], xhat, r.inv2[s, j, :, 0:1]
        )
        r.middle[part_rows(j)] = grad_middle
        branch = grad_middle.astype(LOW)
        r.brn[s, j, mine] = branch
        gather_start(r.brn, s, 3, j)
        r.norm_part[s, 2:3] += column_sum(grad * xhat)
        r.norm_part[s, 3:4] += column_sum(grad)
        r.norm_part[s, 4:5] += column_sum(branch)

    def mixed_back(s, j):
        gather_wait(r.brn, s, 3, j)
        place = place_of(c * local + j * stream_rows + iota((stream_rows, 1), 0))
        r.gmix[j] = (dot_nt(r.brn[s, j], r.wo[s]) * row_mask(place)).astype(LOW)

    def attend_line_back(s):
        grad_q, grad_k, grad_v = [], [], []
        grad_mixed = flat(r.gmix[...])
        queries = flat(r.qry[s])
        for head in range(heads):
            cols = head_cols(head)
            weights = r.soft[s, head]
            grad_head = grad_mixed[:, cols]
            grad_weights = dot_nt(grad_head, r.kv[s, 1, :, cols])
            inner = jnp.sum(weights * grad_weights, axis=-1, keepdims=True)
            grad_scores = (weights * (grad_weights - inner)).astype(LOW)
            grad_k.append(scale * dot_tn(grad_scores, queries[:, cols]))
            grad_v.append(dot_tn(weights.astype(LOW), grad_head))
            grad_q.append(scale * dot_nn(grad_scores, r.kv[s, 0, :, cols]))
        r.dkv_all[0] = jnp.concatenate(grad_k, axis=-1)
        r.dkv_all[1] = jnp.concatenate(grad_v, axis=-1)
        r.dkv_out[s] = r.dkv_all[:, row_block(1 - c, local)].astype(LOW)
        dkv_copy(s).start()
        grad_q = jnp.concatenate(grad_q, axis=-1).astype(LOW)
        r.dqkv[s, 0] = grad_q.reshape(r.dqkv.shape[2:])
        r.norm_part[s, 7:8, :head_width] = column_sum(grad_q)
        dkv_copy(s).wait_recv()
        for which in range(2):
            joined = r.dkv_all[which, my_half] + r.dkv_in[s, which].astype(F32)
            joined = joined.astype(LOW)
            r.dqkv[s, 1 + which] = joined.reshape(r.dqkv.shape[2:])
            if which == 1:
                r.norm_part[s, 7:8, half_width : half_width + head_width] = column_sum(joined)

    def leave_back(s, j):
        product = dot_nn(r.dqkv[s, 0, j], r.wq[s, 0:head_width])
        for which in range(1, 3):
            weight = r.wq[s, which * head_width : (which + 1) * head_width]
            product = product + dot_nn(r.dqkv[s, which, j], weight)
        scatter_start(s, 3, j, product)

    def finish_back(s, j):
        grad = scatter_sum(s, 3, j)
        xhat = r.xhat1[s, j]
        result = r.middle[part_rows(j)] + standard_back(
            grad * r.small[s, 0:1], xhat, r.inv1[s, j, :, 0:1]
        )
        r.upstream[part_rows(j)] = result.astype(LOW)
        r.grad_low[s, part_rows(j)] = result.astype(LOW)
        r.norm_part[s, 0:1] += column_sum(grad * xhat)
        r.norm_part[s, 1:2] += column_sum(grad)

    for j in streams:
        turn(lines - 1, j)

    def backward(index, _):
        s = lines - 1 - index
        for j in streams:
            feed_back(s, j)
        rows_start(UPS, s)
        rows_start(GPRE, s)
        for j in streams:
            between_back(s, j)
        for j in streams:
            mixed_back(s, j)
        rows_start(BRN, s)
        attend_line_back(s)
        for j in streams:
            leave_back(s, j)
        rows_start(DQKV, s)
        for j in streams:
            finish_back(s, j)

            @pl.when(s > 0)
            def _():
                turn(s - 1, j)

        home_start(*norm_home, s)
        home_start(*grad_home, s)
        return 0

    lax.fori_loop(0, lines, backward, 0)

    drain(r.norm_all, r.norm_r)
    slot = c * chips + t
    norm_sum = r.norm_all[0]
    for line in range(1, lines):
        norm_sum = norm_sum + r.norm_all[line]
    r.ends[slot] = norm_sum

    def ends_copy(step):
        core, chip = step // chips, step % chips
        view = r.ends.at[slot]
        return remote(
            view,
            view,
            r.ends_s.at[step - 1],
            r.ends_r,
            seq=(c + core) % 2,
            tensor=(t + chip) % chips,
        )

    for step in range(1, 2 * chips):
        ends_copy(step).start()

    for index in range(8):
        drain(all_rows[index], r.rows_r.at[index])
    drain(r.acts, r.out_r)
    drain(r.grads, r.grad_r)
    drain(r.ends.at[0 : 2 * chips - 1], r.ends_r)
    for step in range(1, 2 * chips):
        ends_copy(step).wait_send()
    for step in range(1, lines):
        small_copy(step - 1, (a + step) % lines, a).wait_send()
        count_copy(step - 1, (a + step) % lines, a).wait_send()
    for p in range(4):
        for which, line in enumerate((beside(a), above(a))):
            first_hop(p, a, line, which).wait_send()

    def sent(s, _):
        home_sent(*out_home, s)
        home_sent(*grad_home, s)
        home_sent(*norm_home, s)
        kv_copy(s, c).wait_send()
        dkv_copy(s).wait_send()
        for index in range(8):
            rows_sent(index, s)
        for p in range(4):

            @pl.when((a == beside(s)) | (a == above(s)))
            def _():
                second_hop(p, s, 0).wait_send()

            @pl.when(a != s)
            def _():
                core_hop(p, s, c).wait_send()

        return 0

    lax.fori_loop(0, lines, sent, 0)


def relay_call(inputs, cotangent, lengths, chosen, singles, weights):
    lines = lax.axis_size("section")
    chips = lax.axis_size("tensor")
    rows, buckets, width = inputs.shape[1:]
    local, total, half = rows * chips, 2 * rows * chips, width // 2
    head_width, units = weights["wo_in"].shape[0], weights["wp_in"].shape[0]
    heads = head_width // HDIM
    sub, stream = rows // STREAMS, local // STREAMS
    peers = chips - 1
    vmem, dma = pltpu.VMEM, pltpu.SemaphoreType.DMA
    operands = dict(
        inputs=inputs,
        cotangent=cotangent,
        lengths=lengths,
        chosen=chosen,
        **singles,
        **weights,
    )

    def space(name):
        if name in weights:
            return pl.ANY
        return pltpu.SMEM if operands[name] is lengths else pltpu.VMEM

    sums = dict(
        acts=((lines, rows, width), LOW),
        grads=((lines, rows, width), LOW),
        ends=((2 * chips, 8, width), F32),
    )
    gathered = dict(
        all_nrm=((lines, 2, STREAMS, stream, half), LOW),
        all_nmlp=((lines, 2, STREAMS, stream, half), LOW),
        all_ups=((lines, 2, STREAMS, stream, half), LOW),
        all_brn=((lines, 2, STREAMS, stream, half), LOW),
        all_act=((lines, 2, STREAMS, stream, units), LOW),
        all_gpre=((lines, 2, STREAMS, stream, units), LOW),
        all_mix=((lines, 2, STREAMS, stream, head_width), LOW),
        all_dqkv=((lines, 2, 3, STREAMS, stream, head_width), LOW),
    )
    outputs = dict(**sums, **gathered)
    scratch = dict(
        wq=vmem((lines,) + weights["wq_in"].shape, LOW),
        wo=vmem((lines,) + weights["wo_in"].shape, LOW),
        wf=vmem((lines,) + weights["wf_in"].shape, LOW),
        wp=vmem((lines,) + weights["wp_in"].shape, LOW),
        small_own=vmem((8, width), F32),
        small=vmem((lines, 8, width), F32),
        count_own=vmem((lines, 8, total), F32),
        count=vmem((lines, 8, total), F32),
        hidden=vmem((rows, width), F32),
        middle=vmem((rows, width), F32),
        upstream=vmem((rows, width), LOW),
        xhat1=vmem((lines, STREAMS, sub, width), F32),
        inv1=vmem((lines, STREAMS, sub, 128), F32),
        xhat2=vmem((lines, STREAMS, sub, width), F32),
        inv2=vmem((lines, STREAMS, sub, 128), F32),
        nrm=vmem((lines, STREAMS, stream, width), LOW),
        nmlp=vmem((lines, STREAMS, stream, width), LOW),
        ups=vmem((lines, STREAMS, stream, width), LOW),
        brn=vmem((lines, STREAMS, stream, width), LOW),
        act=vmem((lines, STREAMS, stream, units), LOW),
        gpre=vmem((lines, STREAMS, stream, units), LOW),
        slope=vmem((lines, STREAMS, stream, units), F32),
        mix=vmem((lines, STREAMS, stream, head_width), LOW),
        qry=vmem((lines, STREAMS, stream, head_width), LOW),
        gmix=vmem((STREAMS, stream, head_width), LOW),
        dqkv=vmem((lines, 3, STREAMS, stream, head_width), LOW),
        kv=vmem((lines, 2, total, head_width), LOW),
        soft=vmem((lines, heads, local, total), F32),
        dkv_all=vmem((2, total, head_width), F32),
        dkv_out=vmem((lines, 2, local, head_width), LOW),
        dkv_in=vmem((lines, 2, local, head_width), LOW),
        part=vmem((4, STREAMS, stream, width), LOW),
        arrived=vmem((lines, 4, STREAMS, peers, sub, width), LOW),
        out_low=vmem((lines, rows, width), LOW),
        grad_low=vmem((lines, rows, width), LOW),
        norm_part=vmem((lines, 8, width), F32),
        norm_all=vmem((lines, 8, width), F32),
        w_first_s=dma((4, 2)),
        w_first_r=dma((lines, 4)),
        w_second_s=dma((lines, 4)),
        w_second_r=dma((lines, 4, 2)),
        w_core_s=dma((lines, 4)),
        w_core_r=dma((lines, 4)),
        w_own=dma((4,)),
        small_s=dma((lines - 1,)),
        small_r=dma((lines,)),
        count_s=dma((lines - 1,)),
        count_r=dma((lines,)),
        ag_s=dma((4, STREAMS, peers)),
        ag_r=dma((4, STREAMS, peers)),
        rs_s=dma((4, STREAMS, peers)),
        rs_r=dma((4, STREAMS, peers)),
        kv_s=dma((lines,)),
        kv_r=dma((lines,)),
        dkv_s=dma((lines,)),
        dkv_r=dma((lines,)),
        rows_s=dma((8, lines, 2)),
        rows_r=dma((8,)),
        out_s=dma((lines,)),
        out_r=dma,
        grad_s=dma((lines,)),
        grad_r=dma,
        norm_s=dma((lines,)),
        norm_r=dma,
        ends_s=dma((2 * chips - 1,)),
        ends_r=dma,
    )
    names = tuple(operands) + tuple(outputs) + tuple(scratch)
    results = pl.pallas_call(
        functools.partial(relay_kernel, names),
        out_shape=[jax.ShapeDtypeStruct(shape, kind) for shape, kind in outputs.values()],
        in_specs=[pl.BlockSpec(memory_space=space(name)) for name in operands],
        out_specs=[
            pl.BlockSpec(memory_space=pl.ANY if name in gathered else pltpu.VMEM)
            for name in outputs
        ],
        scratch_shapes=list(scratch.values()),
        compiler_params=pltpu.CompilerParams(
            collective_id=0, has_side_effects=True, vmem_limit_bytes=60 * 2**20
        ),
        name="relay",
    )(*operands.values())
    return dict(zip(outputs, results))


def weights_kernel(names, *refs):
    r = types.SimpleNamespace(**dict(zip(names, refs)))
    step = pl.program_id(0)
    micro_count, rows, buckets, width = r.activations.shape
    chips, units, head_width = r.ends.shape[0] // 2, r.all_act.shape[-1], r.all_mix.shape[-1]

    @pl.when(step == 0)
    def _():
        sums = r.ends[0]
        for other in range(1, 2 * chips):
            sums = sums + r.ends[other]
        singles = (r.ln1_gain, r.ln1_shift, r.ln2_gain, r.ln2_shift, r.b_out, r.b_proj)
        for place, single in enumerate(singles):
            single[...] = sums[place : place + 1]
        for chip in range(chips):
            both = r.ends[chip] + r.ends[chips + chip]
            r.b_fc[:, chip * units : (chip + 1) * units] = both[6:7, :units]
            here = slice(chip * head_width, (chip + 1) * head_width)
            r.b_qv[0:1, here] = both[7:8, :head_width]
            r.b_qv[1:2, here] = both[7:8, width // 2 : width // 2 + head_width]
        for target, source in ((r.activations, r.acts), (r.in_grads, r.grads)):
            for micro in range(micro_count):
                rows_of = [
                    source[micro * buckets + bucket].astype(F32)[:, None, :]
                    for bucket in range(buckets)
                ]
                target[micro] = jnp.concatenate(rows_of, axis=1).astype(LOW)
        for target in (r.w_qkv, r.w_out, r.w_fc, r.w_proj):
            target[...] = jnp.zeros_like(target)

    def rows_of_sequence(ref):
        return ref[0].reshape(2 * chips * rows, ref.shape[-1])

    nrm, nmlp, ups, brn, act, gpre, mix = (
        rows_of_sequence(ref)
        for ref in (r.all_nrm, r.all_nmlp, r.all_ups, r.all_brn, r.all_act, r.all_gpre, r.all_mix)
    )
    r.w_proj[...] += dot_tn(act, ups)
    r.w_fc[...] += dot_tn(nmlp, gpre)
    r.w_out[...] += dot_tn(mix, brn)
    for which in range(3):
        grad = r.all_dqkv[0, :, which].reshape(2 * chips * rows, head_width)
        r.w_qkv[which] += dot_tn(grad, nrm)


def weights_call(relayed, inputs_shape, head_width, units):
    lines = lax.axis_size("section")
    chips = lax.axis_size("tensor")
    width = inputs_shape[-1]
    half = width // 2
    outputs = dict(
        activations=(inputs_shape, LOW),
        in_grads=(inputs_shape, LOW),
        ln1_gain=((1, width), F32),
        ln1_shift=((1, width), F32),
        w_qkv=((3, head_width, half), F32),
        b_qv=((2, width), F32),
        w_out=((head_width, half), F32),
        b_out=((1, width), F32),
        ln2_gain=((1, width), F32),
        ln2_shift=((1, width), F32),
        w_fc=((half, units), F32),
        b_fc=((1, chips * units), F32),
        w_proj=((units, half), F32),
        b_proj=((1, width), F32),
    )

    def spec(array):
        if len(array.shape) < 5:
            return pl.BlockSpec(array.shape, lambda step: (0,) * len(array.shape))
        return pl.BlockSpec(
            (1,) + array.shape[1:], lambda step: (step,) + (0,) * (len(array.shape) - 1)
        )

    def whole(shape):
        return pl.BlockSpec(shape, lambda step: (0,) * len(shape))

    return pl.pallas_call(
        functools.partial(weights_kernel, tuple(relayed) + tuple(outputs)),
        out_shape=[jax.ShapeDtypeStruct(shape, kind) for shape, kind in outputs.values()],
        grid=(lines,),
        in_specs=[spec(array) for array in relayed.values()],
        out_specs=[whole(shape) for shape, _ in outputs.values()],
        compiler_params=pltpu.CompilerParams(vmem_limit_bytes=48 * 2**20),
        name="weight_gradients",
    )(*relayed.values())


def on_line(
    inputs,
    cotangent,
    lengths,
    chosen,
    ln1_gain,
    ln1_shift,
    w_qkv,
    b_qv,
    w_out,
    b_out,
    ln2_gain,
    ln2_shift,
    w_fc,
    b_fc,
    w_proj,
    b_proj,
):
    head_width, units = w_out.shape[1], w_fc.shape[2]
    singles = dict(
        ln1_gain=ln1_gain,
        ln1_shift=ln1_shift,
        ln2_gain=ln2_gain,
        ln2_shift=ln2_shift,
        b_out=b_out,
        b_proj=b_proj,
        b_fc=b_fc,
        b_qv=b_qv[0],
    )
    weights = dict(
        wq_in=jnp.swapaxes(w_qkv[0], 1, 2).reshape(-1, inputs.shape[-1]),
        wo_in=w_out[0],
        wf_in=w_fc[0],
        wp_in=w_proj[0],
    )
    picks = chosen.reshape((-1,) + chosen.shape[-2:])
    relayed = relay_call(inputs, cotangent, lengths, picks, singles, weights)
    results = list(weights_call(relayed, inputs.shape, head_width, units))
    results[4] = jnp.swapaxes(results[4], 1, 2)
    vectors = (2, 3, 7, 8, 9, 11, 13)
    return tuple(
        result if place in vectors else result[None] for place, result in enumerate(results)
    )


def fits_lines(mesh):
    return mesh.shape["section"] == 4 and mesh.shape["seq"] == 2 and mesh.shape["tensor"] == 4


def solution(mesh):
    placed = (
        P(None, ("seq", "tensor"), None, None),
        P(None, ("seq", "tensor"), None, None),
        P(),
        P("section", None, None, "tensor", "seq", None),
        P("section", None),
        P("section", None),
        P("section", None, None, "tensor"),
        P("section", None, "tensor"),
        P("section", "tensor", None),
        P("section", None),
        P("section", None),
        P("section", None),
        P("section", None, "tensor"),
        P("section", "tensor"),
        P("section", "tensor", None),
        P("section", None),
    )
    return jax.shard_map(
        on_line if fits_lines(mesh) else on_device,
        mesh=mesh,
        in_specs=placed,
        out_specs=(
            P("section", None, ("seq", "tensor"), None, None),
            P("section", None, ("seq", "tensor"), None, None),
            P("section", None),
            P("section", None),
            P("section", None, "seq", "tensor"),
            P("section", None, None),
            P("section", "tensor", "seq"),
            P("section", None),
            P("section", None),
            P("section", None),
            P("section", "seq", "tensor"),
            P("section", None),
            P("section", "tensor", "seq"),
            P("section", None),
        ),
        check_vma=False,
    )
```

```python
import functools
import types

import jax
import jax.numpy as jnp
from jax import lax
from jax.experimental import pallas as pl
from jax.experimental.pallas import tpu as pltpu
from jax.sharding import PartitionSpec as P

HDIM = 64
WIN = 64
QB = 64
KSEL = 64


NORM_EPS = 1e-05
MASKED = -1000000000.0


def from_behind(value, axis, steps):
    count = lax.axis_size(axis)
    first, last = (max(0, -steps), min(count, count - steps))
    return lax.ppermute(value, axis, [(source, source + steps) for source in range(first, last)])


def layer_norm(values, gain, shift):
    average = jnp.mean(values, axis=-1, keepdims=True)
    centred = values - average
    variance = jnp.mean(centred * centred, axis=-1, keepdims=True)
    return centred * lax.rsqrt(variance + NORM_EPS) * gain + shift


def gelu_tanh(values):
    return (
        0.5
        * values
        * (1.0 + jnp.tanh(0.7978845608028654 * (values + 0.044715 * values * values * values)))
    )


def gather_rows(row_block):
    return lax.all_gather(row_block, "tensor", axis=0, tiled=True)


def scatter_product(left_rows, weight, formula):
    return lax.psum_scatter(
        jnp.einsum(formula, left_rows, weight, preferred_element_type=jnp.float32).astype(
            jnp.bfloat16
        ),
        "tensor",
        scatter_dimension=0,
        tiled=True,
    ).astype(jnp.float32)


def near_slabs(full_rows, seq_start, seq_first, length_local):
    buckets = full_rows.shape[1]
    heads_local = full_rows.shape[2] // HDIM
    blocks = length_local // QB
    earlier = lax.dynamic_slice_in_dim(full_rows, jnp.maximum(seq_start - WIN, 0), WIN, 0)
    earlier = jnp.where(seq_first, jnp.zeros_like(earlier), earlier)
    local_part = lax.dynamic_slice_in_dim(full_rows, seq_start, length_local, 0)
    segment = jnp.concatenate([earlier, local_part], 0).reshape(
        length_local + WIN, buckets, heads_local, HDIM
    )
    return jnp.concatenate(
        [
            segment[offset_index * QB : offset_index * QB + length_local].reshape(
                blocks, QB, buckets, heads_local, HDIM
            )
            for offset_index in range(WIN // QB + 1)
        ],
        1,
    )


def far_rows(full_rows, flat_index):
    total_rows, buckets, feature_width = full_rows.shape
    heads_local = feature_width // HDIM
    return jnp.take(full_rows.reshape(total_rows * buckets * heads_local, HDIM), flat_index, axis=0)


def key_geometry(chosen_now, seq_start, blocks):
    buckets, heads_local = (chosen_now.shape[0], chosen_now.shape[1])
    bucket_ids = lax.broadcasted_iota(jnp.int32, chosen_now.shape, 0)
    head_ids = lax.broadcasted_iota(jnp.int32, chosen_now.shape, 1)
    flat_index = (chosen_now * buckets + bucket_ids) * heads_local + head_ids
    block_start = seq_start + QB * lax.broadcasted_iota(jnp.int32, (blocks, 1, 1), 0)
    query_ids = lax.broadcasted_iota(jnp.int32, (1, QB, 1), 1)
    key_ids = lax.broadcasted_iota(jnp.int32, (1, 1, WIN + QB), 2)
    distance = query_ids + WIN - key_ids
    near_ok = (distance >= 0) & (distance < WIN) & (block_start + key_ids - WIN >= 0)
    far_ok = chosen_now + WIN <= block_start.reshape(1, 1, blocks, 1)
    near_mask = jnp.broadcast_to(
        near_ok[:, None, None], (blocks, buckets, heads_local, QB, WIN + QB)
    )
    far_mask = jnp.broadcast_to(
        jnp.transpose(far_ok, (2, 0, 1, 3))[:, :, :, None, :],
        (blocks, buckets, heads_local, QB, KSEL),
    )
    return (flat_index, jnp.concatenate([near_mask, far_mask], -1))


def attention_setup(queries, key_rows, value_rows, chosen_now, seq_start, seq_first):
    length_local, buckets, feature_width = queries.shape
    heads_local = feature_width // HDIM
    blocks = length_local // QB
    query_blocks = queries.reshape(blocks, QB, buckets, heads_local, HDIM)
    flat_index, key_mask = key_geometry(chosen_now, seq_start, blocks)
    near_keys = near_slabs(key_rows, seq_start, seq_first, length_local)
    near_values = near_slabs(value_rows, seq_start, seq_first, length_local)
    far_keys = far_rows(key_rows, flat_index)
    far_values = far_rows(value_rows, flat_index)
    near_scores = jnp.einsum(
        "bqnhe,btnhe->bnhqt", query_blocks, near_keys, preferred_element_type=jnp.float32
    )
    far_scores = jnp.einsum(
        "bqnhe,nhbke->bnhqk", query_blocks, far_keys, preferred_element_type=jnp.float32
    )
    scores = jnp.where(
        key_mask, HDIM ** (-0.5) * jnp.concatenate([near_scores, far_scores], -1), MASKED
    )
    return (query_blocks, near_keys, near_values, far_keys, far_values, flat_index, scores)


def attend(queries, key_rows, value_rows, chosen_now, seq_start, seq_first):
    query_blocks, near_keys, near_values, far_keys, far_values, flat_index, scores = (
        attention_setup(queries, key_rows, value_rows, chosen_now, seq_start, seq_first)
    )
    span = WIN + QB
    row_top = jnp.max(scores, -1, keepdims=True)
    exp_terms = jnp.exp(scores - row_top)
    row_total = jnp.sum(exp_terms, -1, keepdims=True)
    softmax_low = (exp_terms / row_total).astype(jnp.bfloat16)
    near_part = jnp.einsum(
        "bnhqt,btnhe->bqnhe",
        softmax_low[..., :span],
        near_values,
        preferred_element_type=jnp.float32,
    )
    far_part = jnp.einsum(
        "bnhqk,nhbke->bqnhe",
        softmax_low[..., span:],
        far_values,
        preferred_element_type=jnp.float32,
    )
    return ((near_part + far_part).reshape(queries.shape), row_top + jnp.log(row_total))


def spread_back(near_grad, far_grad, flat_index, seq_start, seq_first, total_rows):
    blocks, span, buckets, heads_local, head_size = near_grad.shape
    length_local = blocks * QB
    feature_width = heads_local * head_size
    segment = jnp.zeros((length_local + WIN, buckets, heads_local, head_size), jnp.float32)
    for offset_index in range(WIN // QB + 1):
        piece = near_grad[:, offset_index * QB : (offset_index + 1) * QB].reshape(
            length_local, buckets, heads_local, head_size
        )
        segment = segment.at[offset_index * QB : offset_index * QB + length_local].add(piece)
    full_rows = jnp.zeros((total_rows * buckets * heads_local, head_size), jnp.float32)
    full_rows = full_rows.at[flat_index.reshape(-1)].add(far_grad.reshape(-1, head_size))
    full_rows = full_rows.reshape(total_rows, buckets, feature_width)
    local_part = segment[WIN:].reshape(length_local, buckets, feature_width)
    earlier = jnp.where(seq_first, 0.0, segment[:WIN].reshape(WIN, buckets, feature_width))
    full_rows = lax.dynamic_update_slice_in_dim(
        full_rows,
        lax.dynamic_slice_in_dim(full_rows, seq_start, length_local, 0) + local_part,
        seq_start,
        0,
    )
    earlier_start = jnp.maximum(seq_start - WIN, 0)
    full_rows = lax.dynamic_update_slice_in_dim(
        full_rows,
        lax.dynamic_slice_in_dim(full_rows, earlier_start, WIN, 0) + earlier,
        earlier_start,
        0,
    )
    return full_rows


def attend_back(
    queries, key_rows, value_rows, chosen_now, seq_start, seq_first, log_total, grad_mixed
):
    query_blocks, near_keys, near_values, far_keys, far_values, flat_index, scores = (
        attention_setup(queries, key_rows, value_rows, chosen_now, seq_start, seq_first)
    )
    span = WIN + QB
    score_scale = HDIM ** (-0.5)
    grad_blocks = grad_mixed.reshape(query_blocks.shape)
    weights_full = jnp.exp(scores - log_total)
    softmax_low = weights_full.astype(jnp.bfloat16)
    grad_near_weights = jnp.einsum(
        "bqnhe,btnhe->bnhqt", grad_blocks, near_values, preferred_element_type=jnp.float32
    )
    grad_far_weights = jnp.einsum(
        "bqnhe,nhbke->bnhqk", grad_blocks, far_values, preferred_element_type=jnp.float32
    )
    grad_weights = jnp.concatenate([grad_near_weights, grad_far_weights], -1)
    row_dot = jnp.sum(weights_full * grad_weights, -1, keepdims=True)
    grad_scores = (weights_full * (grad_weights - row_dot)).astype(jnp.bfloat16)
    grad_near, grad_far = (grad_scores[..., :span], grad_scores[..., span:])
    grad_queries = score_scale * (
        jnp.einsum("bnhqt,btnhe->bqnhe", grad_near, near_keys, preferred_element_type=jnp.float32)
        + jnp.einsum("bnhqk,nhbke->bqnhe", grad_far, far_keys, preferred_element_type=jnp.float32)
    )
    near_key_grad = score_scale * jnp.einsum(
        "bnhqt,bqnhe->btnhe", grad_near, query_blocks, preferred_element_type=jnp.float32
    )
    far_key_grad = score_scale * jnp.einsum(
        "bnhqk,bqnhe->nhbke", grad_far, query_blocks, preferred_element_type=jnp.float32
    )
    near_value_grad = jnp.einsum(
        "bnhqt,bqnhe->btnhe",
        softmax_low[..., :span],
        grad_blocks,
        preferred_element_type=jnp.float32,
    )
    far_value_grad = jnp.einsum(
        "bnhqk,bqnhe->nhbke",
        softmax_low[..., span:],
        grad_blocks,
        preferred_element_type=jnp.float32,
    )
    total_rows = key_rows.shape[0]
    key_grad = spread_back(
        near_key_grad, far_key_grad, flat_index, seq_start, seq_first, total_rows
    )
    value_grad = spread_back(
        near_value_grad, far_value_grad, flat_index, seq_start, seq_first, total_rows
    )
    return (grad_queries.reshape(queries.shape), key_grad, value_grad)


def forward_pass(hidden, params, chosen_now, query_mask, seq_start, seq_first, finish):
    (
        ln1_gain,
        ln1_shift,
        w_qkv,
        b_qv,
        w_out,
        b_out,
        ln2_gain,
        ln2_shift,
        w_fc,
        b_fc,
        w_proj,
        b_proj,
    ) = params
    hidden_wide = hidden.astype(jnp.float32)
    normed_all = gather_rows(layer_norm(hidden_wide, ln1_gain, ln1_shift).astype(jnp.bfloat16))
    projected = jnp.einsum("pnd,jdc->jpnc", normed_all, w_qkv, preferred_element_type=jnp.float32)
    queries = (projected[0] + b_qv[0]).astype(jnp.bfloat16)
    key_rows, value_rows = (
        lax.all_gather(projected[1].astype(jnp.bfloat16), "seq", axis=0, tiled=True),
        lax.all_gather((projected[2] + b_qv[1]).astype(jnp.bfloat16), "seq", axis=0, tiled=True),
    )
    attended, log_total = attend(queries, key_rows, value_rows, chosen_now, seq_start, seq_first)
    mixed_rows = (attended * query_mask[:, :, None]).astype(jnp.bfloat16)
    middle = hidden_wide + scatter_product(mixed_rows, w_out, "pnc,cd->pnd") + b_out
    normed_mlp = gather_rows(layer_norm(middle, ln2_gain, ln2_shift).astype(jnp.bfloat16))
    pre_active = (
        jnp.einsum("pnd,df->pnf", normed_mlp, w_fc, preferred_element_type=jnp.float32) + b_fc
    )
    active = gelu_tanh(pre_active).astype(jnp.bfloat16)
    if not finish:
        return (
            normed_all,
            queries,
            key_rows,
            value_rows,
            log_total,
            mixed_rows,
            middle,
            normed_mlp,
            pre_active,
            active,
        )
    output = (middle + scatter_product(active, w_proj, "pnf,fd->pnd") + b_proj).astype(jnp.bfloat16)
    return (output, (key_rows, value_rows))


def backward_pass(hidden, upstream, params, chosen_now, query_mask, seq_start, seq_first):
    (
        ln1_gain,
        ln1_shift,
        w_qkv,
        b_qv,
        w_out,
        b_out,
        ln2_gain,
        ln2_shift,
        w_fc,
        b_fc,
        w_proj,
        b_proj,
    ) = params
    (
        normed_all,
        queries,
        key_rows,
        value_rows,
        log_total,
        mixed_rows,
        middle,
        normed_mlp,
        pre_active,
        active,
    ) = forward_pass(hidden, params, chosen_now, query_mask, seq_start, seq_first, False)
    upstream_all = gather_rows(upstream)
    grad_w_proj = jnp.einsum(
        "pnf,pnd->fd", active, upstream_all, preferred_element_type=jnp.float32
    )
    grad_b_proj = jnp.sum(upstream.astype(jnp.float32), axis=(0, 1))
    grad_active = jnp.einsum(
        "pnd,fd->pnf", upstream_all, w_proj, preferred_element_type=jnp.float32
    )
    unused_value, gelu_pull = jax.vjp(gelu_tanh, pre_active)
    grad_pre = gelu_pull(grad_active)[0].astype(jnp.bfloat16)
    grad_w_fc = jnp.einsum("pnd,pnf->df", normed_mlp, grad_pre, preferred_element_type=jnp.float32)
    grad_b_fc = jnp.sum(grad_pre.astype(jnp.float32), axis=(0, 1))
    grad_normed_mlp = scatter_product(grad_pre, w_fc, "pnf,df->pnd")
    unused_norm, second_pull = jax.vjp(layer_norm, middle, ln2_gain, ln2_shift)
    grad_mid_norm, grad_ln2_gain, grad_ln2_shift = second_pull(grad_normed_mlp)
    grad_middle = upstream.astype(jnp.float32) + grad_mid_norm
    grad_branch = grad_middle.astype(jnp.bfloat16)
    grad_b_out = jnp.sum(grad_branch.astype(jnp.float32), axis=(0, 1))
    branch_all = gather_rows(grad_branch)
    grad_w_out = jnp.einsum(
        "pnc,pnd->cd", mixed_rows, branch_all, preferred_element_type=jnp.float32
    )
    grad_mixed = jnp.einsum(
        "pnd,cd->pnc", branch_all, w_out, preferred_element_type=jnp.float32
    ).astype(jnp.bfloat16) * query_mask[:, :, None].astype(jnp.bfloat16)
    grad_queries, key_grad_all, value_grad_all = attend_back(
        queries, key_rows, value_rows, chosen_now, seq_start, seq_first, log_total, grad_mixed
    )
    key_grad, value_grad = (
        lax.psum_scatter(
            key_grad_all.astype(jnp.bfloat16), "seq", scatter_dimension=0, tiled=True
        ).astype(jnp.float32),
        lax.psum_scatter(
            value_grad_all.astype(jnp.bfloat16), "seq", scatter_dimension=0, tiled=True
        ).astype(jnp.float32),
    )
    grad_project = jnp.stack(
        [
            grad_queries.astype(jnp.bfloat16),
            key_grad.astype(jnp.bfloat16),
            value_grad.astype(jnp.bfloat16),
        ],
        2,
    )
    grad_w_qkv = jnp.einsum(
        "pnd,pnjc->jdc", normed_all, grad_project, preferred_element_type=jnp.float32
    )
    grad_b_qv = jnp.sum(grad_project[:, :, 0::2].astype(jnp.float32), axis=(0, 1))
    grad_normed = scatter_product(grad_project, w_qkv, "pnjc,jdc->pnd")
    unused_first, first_pull = jax.vjp(layer_norm, hidden.astype(jnp.float32), ln1_gain, ln1_shift)
    grad_in_norm, grad_ln1_gain, grad_ln1_shift = first_pull(grad_normed)
    grad_hidden = (grad_middle + grad_in_norm).astype(jnp.bfloat16)
    block_grads = (
        grad_ln1_gain,
        grad_ln1_shift,
        grad_w_qkv,
        grad_b_qv,
        grad_w_out,
        grad_b_out,
        grad_ln2_gain,
        grad_ln2_shift,
        grad_w_fc,
        grad_b_fc,
        grad_w_proj,
        grad_b_proj,
    )
    return (grad_hidden, block_grads)


def on_device(
    inputs,
    cotangent,
    lengths,
    chosen,
    ln1_gain,
    ln1_shift,
    w_qkv,
    b_qv,
    w_out,
    b_out,
    ln2_gain,
    ln2_shift,
    w_fc,
    b_fc,
    w_proj,
    b_proj,
):
    params = tuple(
        (
            weight_array[0]
            for weight_array in (
                ln1_gain,
                ln1_shift,
                w_qkv,
                b_qv,
                w_out,
                b_out,
                ln2_gain,
                ln2_shift,
                w_fc,
                b_fc,
                w_proj,
                b_proj,
            )
        )
    )
    section_index = lax.axis_index("section")
    section_count = lax.axis_size("section")
    seq_index = lax.axis_index("seq")
    tensor_index = lax.axis_index("tensor")
    tensor_count = lax.axis_size("tensor")
    micro_count, rows_local, buckets, feature_width = inputs.shape
    length_local = rows_local * tensor_count
    heads_width = w_qkv.shape[-1]
    seq_start = seq_index * length_local
    seq_first = seq_index == 0
    positions = seq_start + lax.broadcasted_iota(jnp.int32, (micro_count, length_local, buckets), 1)
    mask_all = (positions < lengths[:, None, :]).astype(jnp.float32)
    mask_rows = lax.dynamic_slice_in_dim(mask_all, tensor_index * rows_local, rows_local, 1)
    step_count = micro_count + section_count - 1
    chosen_section = chosen[0]
    received = jnp.zeros((rows_local, buckets, feature_width), jnp.bfloat16)
    stored = jnp.zeros((micro_count, rows_local, buckets, feature_width), jnp.bfloat16)
    outputs = jnp.zeros_like(stored)
    for step_index in range(step_count):
        micro_index = step_index - section_index
        running = (micro_index >= 0) & (micro_index < micro_count)
        slot_index = jnp.clip(micro_index, 0, micro_count - 1)
        block_in = jnp.where(
            section_index == 0, lax.dynamic_index_in_dim(inputs, slot_index, 0, False), received
        )
        chosen_now = lax.dynamic_index_in_dim(chosen_section, slot_index, 0, False)
        query_mask = lax.dynamic_index_in_dim(mask_all, slot_index, 0, False)
        result, key_pair = forward_pass(
            block_in, params, chosen_now, query_mask, seq_start, seq_first, True
        )
        stored = jnp.where(
            running, lax.dynamic_update_index_in_dim(stored, block_in, slot_index, 0), stored
        )
        outputs = jnp.where(
            running, lax.dynamic_update_index_in_dim(outputs, result, slot_index, 0), outputs
        )
        received = from_behind(result, "section", 1)
    back_received = jnp.zeros((rows_local, buckets, feature_width), jnp.bfloat16)
    in_grads = jnp.zeros_like(stored)
    totals = None
    for step_index in range(step_count):
        micro_index = step_index - (section_count - 1 - section_index)
        running = (micro_index >= 0) & (micro_index < micro_count)
        slot_index = jnp.clip(micro_index, 0, micro_count - 1)
        chosen_now = lax.dynamic_index_in_dim(chosen_section, slot_index, 0, False)
        query_mask = lax.dynamic_index_in_dim(mask_all, slot_index, 0, False)
        local_mask = lax.dynamic_index_in_dim(mask_rows, slot_index, 0, False)
        top_grad = (
            lax.dynamic_index_in_dim(cotangent, slot_index, 0, False).astype(jnp.float32)
            * local_mask[:, :, None]
        ).astype(jnp.bfloat16)
        upstream = jnp.where(section_index == section_count - 1, top_grad, back_received)
        hidden = lax.dynamic_index_in_dim(stored, slot_index, 0, False)
        grad_hidden, block_grads = backward_pass(
            hidden, upstream, params, chosen_now, query_mask, seq_start, seq_first
        )
        block_grads = tuple(
            (jnp.where(running, grad_part, jnp.zeros_like(grad_part)) for grad_part in block_grads)
        )
        totals = (
            block_grads
            if step_index == 0
            else tuple(
                (total_part + grad_part for total_part, grad_part in zip(totals, block_grads))
            )
        )
        in_grads = jnp.where(
            running, lax.dynamic_update_index_in_dim(in_grads, grad_hidden, slot_index, 0), in_grads
        )
        back_received = from_behind(grad_hidden, "section", -1)
    (
        sum_ln1_gain,
        sum_ln1_shift,
        sum_w_qkv,
        sum_b_qv,
        sum_w_out,
        sum_b_out,
        sum_ln2_gain,
        sum_ln2_shift,
        sum_w_fc,
        sum_b_fc,
        sum_w_proj,
        sum_b_proj,
    ) = totals
    part_qkv, part_out, part_fc, part_proj = (
        lax.psum_scatter(
            sum_w_qkv.astype(jnp.bfloat16), "seq", scatter_dimension=1, tiled=True
        ).astype(jnp.float32),
        lax.psum_scatter(
            sum_w_out.astype(jnp.bfloat16), "seq", scatter_dimension=1, tiled=True
        ).astype(jnp.float32),
        lax.psum_scatter(
            sum_w_fc.astype(jnp.bfloat16), "seq", scatter_dimension=0, tiled=True
        ).astype(jnp.float32),
        lax.psum_scatter(
            sum_w_proj.astype(jnp.bfloat16), "seq", scatter_dimension=1, tiled=True
        ).astype(jnp.float32),
    )
    bias_qv = lax.dynamic_update_slice_in_dim(
        jnp.zeros((2, feature_width), jnp.float32), sum_b_qv, tensor_index * heads_width, 1
    )
    units_local = sum_b_fc.shape[0]
    bias_fc = lax.dynamic_update_slice_in_dim(
        jnp.zeros((units_local * tensor_count,), jnp.float32),
        sum_b_fc,
        tensor_index * units_local,
        0,
    )
    small_sums = lax.psum(
        (
            sum_ln1_gain,
            sum_ln1_shift,
            bias_qv,
            sum_b_out,
            sum_ln2_gain,
            sum_ln2_shift,
            bias_fc,
            sum_b_proj,
        ),
        ("seq", "tensor"),
    )
    return (
        outputs[None],
        in_grads[None],
        small_sums[0][None],
        small_sums[1][None],
        part_qkv[None],
        small_sums[2][None],
        part_out[None],
        small_sums[3][None],
        small_sums[4][None],
        small_sums[5][None],
        part_fc[None],
        small_sums[6][None],
        part_proj[None],
        small_sums[7][None],
    )


STREAMS = 2
NRM, NMLP, UPS, BRN, ACT, GPRE, MIX, DQKV = range(8)
F32 = jnp.float32
LOW = jnp.bfloat16
MESH_ID = pl.DeviceIdType.MESH


def dot_nn(left, right):
    return lax.dot_general(left, right, (((1,), (0,)), ((), ())), preferred_element_type=F32)


def dot_nt(left, right):
    return lax.dot_general(left, right, (((1,), (1,)), ((), ())), preferred_element_type=F32)


def dot_tn(left, right):
    return lax.dot_general(left, right, (((0,), (0,)), ((), ())), preferred_element_type=F32)


def standard(rows):
    centred = rows - jnp.mean(rows, axis=-1, keepdims=True)
    scale = lax.rsqrt(jnp.mean(centred * centred, axis=-1, keepdims=True) + NORM_EPS)
    return centred * scale, scale


def standard_back(grad, xhat, scale):
    inner = jnp.mean(grad * xhat, axis=-1, keepdims=True)
    return scale * (grad - jnp.mean(grad, axis=-1, keepdims=True) - xhat * inner)


def column_sum(rows):
    return jnp.sum(rows.astype(F32), axis=0, keepdims=True)


def relay_kernel(names, *refs):
    r = types.SimpleNamespace(**dict(zip(names, refs)))
    a, c, t = (lax.axis_index(name) for name in ("section", "seq", "tensor"))
    lines = lax.axis_size("section")
    chips = lax.axis_size("tensor")
    rows, buckets, width = r.inputs.shape[1:]
    half_width = width // 2
    local = rows * chips
    total = 2 * local
    sub = rows // STREAMS
    stream_rows = local // STREAMS
    head_width = r.wo_in.shape[0]
    heads = head_width // HDIM
    blocks = local // QB
    units = r.wp_in.shape[0]
    scale = HDIM ** (-0.5)
    streams = range(STREAMS)

    def remote(src, dst, send, recv, **target):
        return pltpu.make_async_remote_copy(
            src_ref=src,
            dst_ref=dst,
            send_sem=send,
            recv_sem=recv,
            device_id=target,
            device_id_type=MESH_ID,
        )

    def drain(ref, sem):
        pltpu.make_async_copy(ref, ref, sem).wait()

    def row_block(index, size):
        return pl.ds(pl.multiple_of(index * size, size), size)

    mine = row_block(t, sub)
    my_half = row_block(c, local)

    barrier = pltpu.get_barrier_semaphore()
    for core in range(2):
        for step in range(1, chips):
            there = {"tensor": (t + step) % chips, "seq": core}
            pl.semaphore_signal(barrier, inc=1, device_id=there, device_id_type=MESH_ID)
        for step in range(1, lines):
            there = {"section": (a + step) % lines, "seq": core}
            pl.semaphore_signal(barrier, inc=1, device_id=there, device_id_type=MESH_ID)
    pl.semaphore_signal(barrier, inc=1, device_id={"seq": 1 - c}, device_id_type=MESH_ID)
    pl.semaphore_wait(barrier, 2 * (chips - 1) + 2 * (lines - 1) + 1)

    def beside(s):
        return s + 1 - 2 * (s % 2)

    def above(s):
        return (s + 2) % 4

    def store(p):
        return (r.wq, r.wo, r.wf, r.wp)[p]

    def source(p):
        return (r.wq_in, r.wo_in, r.wf_in, r.wp_in)[p]

    def height(p):
        return source(p).shape[0]

    def core_half(p, s, core):
        return store(p).at[s, row_block(core, height(p) // 2)]

    def first_hop(p, s, neighbour, which):
        return remote(
            source(p).at[row_block(c, height(p) // 2)],
            core_half(p, s, c),
            r.w_first_s.at[p, which],
            r.w_first_r.at[s, p],
            section=neighbour,
        )

    def second_hop(p, s, which):
        view = store(p).at[s, row_block(2 * c + which, height(p) // 4)]
        return remote(
            view, view, r.w_second_s.at[s, p], r.w_second_r.at[s, p, which], section=3 - s
        )

    def core_hop(p, s, core):
        view = core_half(p, s, core)
        return remote(view, view, r.w_core_s.at[s, p], r.w_core_r.at[s, p], seq=1 - c)

    def own_copy(p):
        return pltpu.make_async_copy(source(p), store(p).at[a], r.w_own.at[p])

    def pass_on(s, p):
        for which, line in enumerate((beside(s), above(s))):

            @pl.when(a == line)
            def _():
                first_hop(p, s, line, which).wait_recv()
                second_hop(p, s, which).start()
                core_hop(p, s, c).start()

    def pass_far(s, p):
        @pl.when(a == 3 - s)
        def _():
            second_hop(p, s, 0).wait_recv()
            second_hop(p, s, 1).wait_recv()
            core_hop(p, s, c).start()

    def need(s, p):
        @pl.when(s == 0)
        def _():
            pass_on(s, p)
            pass_far(s, p)

        @pl.when(a == s)
        def _():
            own_copy(p).wait()

        @pl.when(a != s)
        def _():
            core_hop(p, s, 1 - c).wait_recv()

    def small_copy(step, line, slot):
        return remote(
            r.small_own, r.small.at[slot], r.small_s.at[step], r.small_r.at[slot], section=line
        )

    def count_copy(step, line, slot):
        return remote(
            r.count_own.at[line],
            r.count.at[slot],
            r.count_s.at[step],
            r.count_r.at[slot],
            section=line,
        )

    singles = (r.ln1_gain, r.ln1_shift, r.ln2_gain, r.ln2_shift, r.b_out, r.b_proj)
    for place, single in enumerate(singles):
        r.small_own[place : place + 1] = single[...]
    r.small_own[6:7, :units] = r.b_fc[...]
    r.small_own[7:8, :head_width] = r.b_qv[0:1]
    r.small_own[7:8, half_width : half_width + head_width] = r.b_qv[1:2]
    for step in range(1, lines):
        small_copy(step - 1, (a + step) % lines, a).start()
    for p in range(4):
        for which, line in enumerate((beside(a), above(a))):
            first_hop(p, a, line, which).start()
    for p in range(4):
        own_copy(p).start()
    r.small[a] = r.small_own[...]

    def place_of(index):
        inside = index % local
        stream, left = inside // stream_rows, inside % stream_rows
        return (index // local) * local + (left // sub) * rows + stream * sub + left % sub

    def iota(shape, dimension):
        return lax.broadcasted_iota(jnp.int32, shape, dimension)

    square = jnp.where(iota((KSEL, KSEL), 0) == iota((KSEL, KSEL), 1), 1.0, 0.0).astype(LOW)
    position = place_of(iota((KSEL, total), 1)).astype(F32)
    for pair in range(lines * heads):
        line, head = pair // heads, pair % heads
        columns = dot_nt(square, r.chosen[pair].astype(F32).astype(LOW))
        for block in range(blocks):
            pick = head * blocks + block
            r.count_own[line, pick : pick + 1, :] = jnp.sum(
                jnp.where(columns[:, block : block + 1] == position, 1.0, 0.0),
                axis=0,
                keepdims=True,
            )
    for step in range(1, lines):
        count_copy(step - 1, (a + step) % lines, a).start()
    r.count[a] = r.count_own[a]

    partners = (3 - t, (t + 2) % 4, t + 1 - 2 * (t % 2))

    def gather(buffer, s, kind, j, slot, chip):
        view = buffer.at[s, j, row_block(chip, sub)]
        return remote(
            view,
            view,
            r.ag_s.at[kind, j, slot],
            r.ag_r.at[kind, j, slot],
            tensor=partners[slot],
        )

    def gather_start(buffer, s, kind, j):
        for slot in range(chips - 1):
            gather(buffer, s, kind, j, slot, t).start()

    def gather_wait(buffer, s, kind, j):
        for slot in range(chips - 1):
            gather(buffer, s, kind, j, slot, partners[slot]).wait_recv()
        for slot in range(chips - 1):
            gather(buffer, s, kind, j, slot, t).wait_send()

    def scatter(s, kind, j, slot):
        return remote(
            r.part.at[kind, j, row_block(partners[slot], sub)],
            r.arrived.at[s, kind, j, slot],
            r.rs_s.at[kind, j, slot],
            r.rs_r.at[kind, j, slot],
            tensor=partners[slot],
        )

    def scatter_start(s, kind, j, product):
        r.part[kind, j] = product.astype(LOW)
        for slot in range(chips - 1):
            scatter(s, kind, j, slot).start()

    def scatter_sum(s, kind, j):
        result = r.part[kind, j, mine].astype(F32)
        for slot in range(chips - 1):
            scatter(s, kind, j, slot).wait_recv()
            result = result + r.arrived[s, kind, j, slot].astype(F32)
        for slot in range(chips - 1):
            scatter(s, kind, j, slot).wait_send()
        return result

    own_rows = (r.nrm, r.nmlp, r.ups, r.brn, r.act, r.gpre, r.mix, r.dqkv)
    all_rows = (
        r.all_nrm,
        r.all_nmlp,
        r.all_ups,
        r.all_brn,
        r.all_act,
        r.all_gpre,
        r.all_mix,
        r.all_dqkv,
    )

    def rows_copy(index, s, same, stays=False):
        core = c if same else 1 - c
        src = own_rows[index].at[s]
        dst = all_rows[index].at[a, c]
        if index <= BRN:
            src = src.at[:, :, row_block(core, half_width)]
        recv = r.rows_r.at[index]
        if stays:
            return pltpu.make_async_copy(src, dst, recv)
        if same:
            return remote(src, dst, r.rows_s.at[index, s, 0], recv, section=s)
        return remote(src, dst, r.rows_s.at[index, s, 1], recv, section=s, seq=1 - c)

    def rows_start(index, s):
        @pl.when(a == s)
        def _():
            rows_copy(index, s, True, True).start()

        @pl.when(a != s)
        def _():
            rows_copy(index, s, True).start()

        if index <= BRN:
            rows_copy(index, s, False).start()

    def rows_sent(index, s):
        @pl.when(a != s)
        def _():
            rows_copy(index, s, True).wait_send()

        if index <= BRN:
            rows_copy(index, s, False).wait_send()

    def share_copy(index, core):
        view = all_rows[index].at[:, core]
        return remote(view, view, r.share_s.at[index - ACT], r.share_r.at[index - ACT], seq=1 - c)

    def share(index):
        drain(all_rows[index].at[:, c], r.rows_r.at[index])
        share_copy(index, c).start()

    def home_copy(src, dst, send, recv, s):
        return remote(src.at[s], dst.at[a], send.at[s], recv, section=s)

    def home_start(src, dst, send, recv, s):
        @pl.when(a == s)
        def _():
            pltpu.make_async_copy(src.at[s], dst.at[a], recv).start()

        @pl.when(a != s)
        def _():
            home_copy(src, dst, send, recv, s).start()

    def home_sent(*what):
        @pl.when(a != what[-1])
        def _():
            home_copy(*what).wait_send()

    out_home = (r.out_low, r.acts, r.out_s, r.out_r)
    grad_home = (r.grad_low, r.grads, r.grad_s, r.grad_r)
    norm_home = (r.norm_part, r.norm_all, r.norm_s, r.norm_r)

    length = r.lengths[a // buckets, a % buckets]
    query = place_of(c * local + iota((local, total), 0))
    key = place_of(iota((local, total), 1))
    near = jnp.where((query >= key) & (query - key < WIN), 1.0, 0.0)
    key_row = place_of(iota((1, total), 1))
    block_of = place_of(iota((local, total), 0)) // QB
    first_block = jnp.where(block_of == 0, 1.0, 0.0)

    def row_mask(place):
        return jnp.where(place < length, 1.0, 0.0)

    def multiplicity(s, head):
        times = near
        for block in range(blocks):
            pick = head * blocks + block
            limit = (c * blocks + block) * QB - WIN
            counted = jnp.where(key_row <= limit, r.count[s, pick : pick + 1, :], 0.0)
            times = times + jnp.where(block_of == block, counted, 0.0)
        return times

    def head_cols(head):
        return slice(head * HDIM, (head + 1) * HDIM)

    def kv_copy(s, core):
        view = r.kv.at[s, :, row_block(core, local)]
        return remote(view, view, r.kv_s.at[s], r.kv_r.at[s], seq=1 - c)

    def dkv_copy(s):
        return remote(r.dkv_out.at[s], r.dkv_in.at[s], r.dkv_s.at[s], r.dkv_r.at[s], seq=1 - c)

    def flat(array):
        return array.reshape(local, array.shape[-1])

    def own_sequence(ref):
        both = ref[a // buckets].astype(F32)
        picked = both[:, 0, :]
        for bucket in range(1, buckets):
            picked = jnp.where(a % buckets == bucket, both[:, bucket, :], picked)
        return picked

    def part_rows(j):
        return slice(j * sub, (j + 1) * sub)

    r.hidden[...] = own_sequence(r.inputs)
    own_place = c * local + t * rows + iota((rows, 1), 0)
    r.upstream[...] = (own_sequence(r.cotangent) * row_mask(own_place)).astype(LOW)
    r.norm_part[...] = jnp.zeros_like(r.norm_part)

    def enter(s, j):
        xhat, inverse = standard(r.hidden[part_rows(j)])
        r.xhat1[s, j] = xhat
        r.inv1[s, j] = jnp.broadcast_to(inverse, (sub, 128))
        r.nrm[s, j, mine] = (xhat * r.small[s, 0:1] + r.small[s, 1:2]).astype(LOW)
        gather_start(r.nrm, s, 0, j)

    def project(s, j):
        gather_wait(r.nrm, s, 0, j)
        normed = r.nrm[s, j]
        place = row_block(c * STREAMS + j, stream_rows)
        bias_v = r.small[s, 7:8, half_width : half_width + head_width]
        key_rows = dot_nt(normed, r.wq[s, head_width : 2 * head_width])
        value_rows = dot_nt(normed, r.wq[s, 2 * head_width : 3 * head_width]) + bias_v
        r.kv[s, 0, place] = key_rows.astype(LOW)
        r.kv[s, 1, place] = value_rows.astype(LOW)

    def ask(s, j):
        queries = dot_nt(r.nrm[s, j], r.wq[s, 0:head_width]) + r.small[s, 7:8, :head_width]
        r.qry[s, j] = queries.astype(LOW)

    def attend_line(s):
        mixed = []
        queries = flat(r.qry[s])
        for head in range(heads):
            times = multiplicity(s, head)
            scores = scale * dot_nt(queries[:, head_cols(head)], r.kv[s, 0, :, head_cols(head)])
            scores = jnp.where(times > 0.0, scores, MASKED)
            top = jnp.max(scores, axis=-1, keepdims=True)
            terms = times * jnp.exp(scores - top)
            weights = terms / jnp.sum(terms, axis=-1, keepdims=True)
            r.soft[s, head] = weights
            mixed.append(dot_nn(weights.astype(LOW), r.kv[s, 1, :, head_cols(head)]))
        mask = row_mask(place_of(c * local + iota((local, 1), 0)))
        mixed = (jnp.concatenate(mixed, axis=-1) * mask).astype(LOW)
        r.mix[s] = mixed.reshape(r.mix.shape[1:])

    def leave_attention(s, j):
        scatter_start(s, 0, j, dot_nn(r.mix[s, j], r.wo[s]))

    def between(s, j):
        middle = r.hidden[part_rows(j)] + scatter_sum(s, 0, j) + r.small[s, 4:5]
        r.middle[part_rows(j)] = middle
        xhat, inverse = standard(middle)
        r.xhat2[s, j] = xhat
        r.inv2[s, j] = jnp.broadcast_to(inverse, (sub, 128))
        r.nmlp[s, j, mine] = (xhat * r.small[s, 2:3] + r.small[s, 3:4]).astype(LOW)
        gather_start(r.nmlp, s, 1, j)

    def feed(s, j):
        gather_wait(r.nmlp, s, 1, j)
        before = dot_nn(r.nmlp[s, j], r.wf[s]) + r.small[s, 6:7, :units]
        bend = jnp.tanh(0.7978845608028654 * (before + 0.044715 * before * before * before))
        r.act[s, j] = (0.5 * before * (1.0 + bend)).astype(LOW)
        r.slope[s, j] = 0.5 * (1.0 + bend) + 0.5 * before * (1.0 - bend * bend) * (
            0.7978845608028654 * (1.0 + 3 * 0.044715 * before * before)
        )

    def leave_feed(s, j):
        scatter_start(s, 1, j, dot_nn(r.act[s, j], r.wp[s]))

    def finish(s, j):
        result = r.middle[part_rows(j)] + scatter_sum(s, 1, j) + r.small[s, 5:6]
        r.out_low[s, part_rows(j)] = result.astype(LOW)
        r.hidden[part_rows(j)] = result.astype(LOW).astype(F32)

    def small_ready(s):
        @pl.when(a != s)
        def _():
            small_copy(0, a, s).wait_recv()

    small_ready(0)
    for j in streams:
        enter(0, j)

    def forward(s, _):
        need(s, 0)
        for j in streams:
            project(s, j)
        kv_copy(s, c).start()
        for j in streams:
            ask(s, j)
        rows_start(NRM, s)

        @pl.when(a != s)
        def _():
            count_copy(0, a, s).wait_recv()

        kv_copy(s, 1 - c).wait_recv()
        attend_line(s)
        need(s, 1)
        for j in streams:
            leave_attention(s, j)
        rows_start(MIX, s)
        for j in streams:
            between(s, j)
        need(s, 2)
        for j in streams:
            feed(s, j)
            if j == 0:
                need(s, 3)
            leave_feed(s, j)
        rows_start(NMLP, s)
        rows_start(ACT, s)

        @pl.when(s + 1 < lines)
        def _():
            small_ready(s + 1)

        for j in streams:
            finish(s, j)

            @pl.when(s + 1 < lines)
            def _():
                enter(s + 1, j)

        home_start(*out_home, s)

        @pl.when(s == 0)
        def _():
            for later in range(1, lines):
                for p in range(4):
                    pass_on(later, p)

        @pl.when(s + 1 < lines)
        def _():
            for p in range(4):
                pass_far(s + 1, p)

        return 0

    lax.fori_loop(0, lines, forward, 0)

    def turn(s, j):
        upstream = r.upstream[part_rows(j)]
        r.ups[s, j, mine] = upstream
        gather_start(r.ups, s, 2, j)
        r.norm_part[s, 5:6] += column_sum(upstream)

    def feed_back(s, j):
        gather_wait(r.ups, s, 2, j)
        grad_pre = (dot_nt(r.ups[s, j], r.wp[s]) * r.slope[s, j]).astype(LOW)
        r.gpre[s, j] = grad_pre
        scatter_start(s, 2, j, dot_nt(grad_pre, r.wf[s]))
        r.norm_part[s, 6:7, :units] += column_sum(grad_pre)

    def between_back(s, j):
        grad = scatter_sum(s, 2, j)
        xhat = r.xhat2[s, j]
        upstream = r.upstream[part_rows(j)].astype(F32)
        grad_middle = upstream + standard_back(
            grad * r.small[s, 2:3], xhat, r.inv2[s, j, :, 0:1]
        )
        r.middle[part_rows(j)] = grad_middle
        branch = grad_middle.astype(LOW)
        r.brn[s, j, mine] = branch
        gather_start(r.brn, s, 3, j)
        r.norm_part[s, 2:3] += column_sum(grad * xhat)
        r.norm_part[s, 3:4] += column_sum(grad)
        r.norm_part[s, 4:5] += column_sum(branch)

    def mixed_back(s, j):
        gather_wait(r.brn, s, 3, j)
        place = place_of(c * local + j * stream_rows + iota((stream_rows, 1), 0))
        r.gmix[j] = (dot_nt(r.brn[s, j], r.wo[s]) * row_mask(place)).astype(LOW)

    def attend_line_back(s):
        grad_q, grad_k, grad_v = [], [], []
        grad_mixed = flat(r.gmix[...])
        queries = flat(r.qry[s])
        for head in range(heads):
            cols = head_cols(head)
            weights = r.soft[s, head]
            grad_head = grad_mixed[:, cols]
            grad_weights = dot_nt(grad_head, r.kv[s, 1, :, cols])
            inner = jnp.sum(weights * grad_weights, axis=-1, keepdims=True)
            grad_scores = (weights * (grad_weights - inner)).astype(LOW)
            grad_k.append(scale * dot_tn(grad_scores, queries[:, cols]))
            grad_v.append(dot_tn(weights.astype(LOW), grad_head))
            grad_q.append(scale * dot_nn(grad_scores, r.kv[s, 0, :, cols]))
        r.dkv_all[0] = jnp.concatenate(grad_k, axis=-1)
        r.dkv_all[1] = jnp.concatenate(grad_v, axis=-1)
        r.dkv_out[s] = r.dkv_all[:, row_block(1 - c, local)].astype(LOW)
        dkv_copy(s).start()
        grad_q = jnp.concatenate(grad_q, axis=-1).astype(LOW)
        r.dqkv[s, 0] = grad_q.reshape(r.dqkv.shape[2:])
        r.norm_part[s, 7:8, :head_width] = column_sum(grad_q)
        dkv_copy(s).wait_recv()
        for which in range(2):
            joined = r.dkv_all[which, my_half] + r.dkv_in[s, which].astype(F32)
            joined = joined.astype(LOW)
            r.dqkv[s, 1 + which] = joined.reshape(r.dqkv.shape[2:])
            if which == 1:
                r.norm_part[s, 7:8, half_width : half_width + head_width] = column_sum(joined)

    def leave_back(s, j):
        product = dot_nn(r.dqkv[s, 0, j], r.wq[s, 0:head_width])
        for which in range(1, 3):
            weight = r.wq[s, which * head_width : (which + 1) * head_width]
            product = product + dot_nn(r.dqkv[s, which, j], weight)
        scatter_start(s, 3, j, product)

    def finish_back(s, j):
        grad = scatter_sum(s, 3, j)
        xhat = r.xhat1[s, j]
        result = r.middle[part_rows(j)] + standard_back(
            grad * r.small[s, 0:1], xhat, r.inv1[s, j, :, 0:1]
        )
        r.upstream[part_rows(j)] = result.astype(LOW)
        r.grad_low[s, part_rows(j)] = result.astype(LOW)
        r.norm_part[s, 0:1] += column_sum(grad * xhat)
        r.norm_part[s, 1:2] += column_sum(grad)

    for j in streams:
        turn(lines - 1, j)

    def backward(index, _):
        s = lines - 1 - index
        for j in streams:
            feed_back(s, j)
        rows_start(UPS, s)
        rows_start(GPRE, s)

        @pl.when(index == 1)
        def _():
            share(ACT)
            share(MIX)

        for j in streams:
            between_back(s, j)
        for j in streams:
            mixed_back(s, j)
        rows_start(BRN, s)
        attend_line_back(s)
        for j in streams:
            leave_back(s, j)
        rows_start(DQKV, s)
        for j in streams:
            finish_back(s, j)

            @pl.when(s > 0)
            def _():
                turn(s - 1, j)

        home_start(*norm_home, s)
        home_start(*grad_home, s)
        return 0

    lax.fori_loop(0, lines, backward, 0)

    share(GPRE)
    share(DQKV)

    drain(r.norm_all, r.norm_r)
    slot = c * chips + t
    norm_sum = r.norm_all[0]
    for line in range(1, lines):
        norm_sum = norm_sum + r.norm_all[line]
    r.ends[slot] = norm_sum

    def ends_copy(step):
        core, chip = step // chips, step % chips
        view = r.ends.at[slot]
        return remote(
            view,
            view,
            r.ends_s.at[step - 1],
            r.ends_r,
            seq=(c + core) % 2,
            tensor=(t + chip) % chips,
        )

    for step in range(1, 2 * chips):
        ends_copy(step).start()

    for index in range(ACT):
        drain(all_rows[index], r.rows_r.at[index])
    for index in range(ACT, 8):
        share_copy(index, 1 - c).wait_recv()
        share_copy(index, c).wait_send()
    drain(r.acts, r.out_r)
    drain(r.grads, r.grad_r)
    drain(r.ends.at[0 : 2 * chips - 1], r.ends_r)
    for step in range(1, 2 * chips):
        ends_copy(step).wait_send()
    for step in range(1, lines):
        small_copy(step - 1, (a + step) % lines, a).wait_send()
        count_copy(step - 1, (a + step) % lines, a).wait_send()
    for p in range(4):
        for which, line in enumerate((beside(a), above(a))):
            first_hop(p, a, line, which).wait_send()

    def sent(s, _):
        home_sent(*out_home, s)
        home_sent(*grad_home, s)
        home_sent(*norm_home, s)
        kv_copy(s, c).wait_send()
        dkv_copy(s).wait_send()
        for index in range(8):
            rows_sent(index, s)
        for p in range(4):

            @pl.when((a == beside(s)) | (a == above(s)))
            def _():
                second_hop(p, s, 0).wait_send()

            @pl.when(a != s)
            def _():
                core_hop(p, s, c).wait_send()

        return 0

    lax.fori_loop(0, lines, sent, 0)


def relay_call(inputs, cotangent, lengths, chosen, singles, weights):
    lines = lax.axis_size("section")
    chips = lax.axis_size("tensor")
    rows, buckets, width = inputs.shape[1:]
    local, total, half = rows * chips, 2 * rows * chips, width // 2
    head_width, units = weights["wo_in"].shape[0], weights["wp_in"].shape[0]
    heads = head_width // HDIM
    sub, stream = rows // STREAMS, local // STREAMS
    peers = chips - 1
    vmem, dma = pltpu.VMEM, pltpu.SemaphoreType.DMA
    operands = dict(
        inputs=inputs,
        cotangent=cotangent,
        lengths=lengths,
        chosen=chosen,
        **singles,
        **weights,
    )

    def space(name):
        if name in weights:
            return pl.ANY
        return pltpu.SMEM if operands[name] is lengths else pltpu.VMEM

    sums = dict(
        acts=((lines, rows, width), LOW),
        grads=((lines, rows, width), LOW),
        ends=((2 * chips, 8, width), F32),
    )
    gathered = dict(
        all_nrm=((lines, 2, STREAMS, stream, half), LOW),
        all_nmlp=((lines, 2, STREAMS, stream, half), LOW),
        all_ups=((lines, 2, STREAMS, stream, half), LOW),
        all_brn=((lines, 2, STREAMS, stream, half), LOW),
        all_act=((lines, 2, STREAMS, stream, units), LOW),
        all_gpre=((lines, 2, STREAMS, stream, units), LOW),
        all_mix=((lines, 2, STREAMS, stream, head_width), LOW),
        all_dqkv=((lines, 2, 3, STREAMS, stream, head_width), LOW),
    )
    outputs = dict(**sums, **gathered)
    scratch = dict(
        wq=vmem((lines,) + weights["wq_in"].shape, LOW),
        wo=vmem((lines,) + weights["wo_in"].shape, LOW),
        wf=vmem((lines,) + weights["wf_in"].shape, LOW),
        wp=vmem((lines,) + weights["wp_in"].shape, LOW),
        small_own=vmem((8, width), F32),
        small=vmem((lines, 8, width), F32),
        count_own=vmem((lines, 8, total), F32),
        count=vmem((lines, 8, total), F32),
        hidden=vmem((rows, width), F32),
        middle=vmem((rows, width), F32),
        upstream=vmem((rows, width), LOW),
        xhat1=vmem((lines, STREAMS, sub, width), F32),
        inv1=vmem((lines, STREAMS, sub, 128), F32),
        xhat2=vmem((lines, STREAMS, sub, width), F32),
        inv2=vmem((lines, STREAMS, sub, 128), F32),
        nrm=vmem((lines, STREAMS, stream, width), LOW),
        nmlp=vmem((lines, STREAMS, stream, width), LOW),
        ups=vmem((lines, STREAMS, stream, width), LOW),
        brn=vmem((lines, STREAMS, stream, width), LOW),
        act=vmem((lines, STREAMS, stream, units), LOW),
        gpre=vmem((lines, STREAMS, stream, units), LOW),
        slope=vmem((lines, STREAMS, stream, units), F32),
        mix=vmem((lines, STREAMS, stream, head_width), LOW),
        qry=vmem((lines, STREAMS, stream, head_width), LOW),
        gmix=vmem((STREAMS, stream, head_width), LOW),
        dqkv=vmem((lines, 3, STREAMS, stream, head_width), LOW),
        kv=vmem((lines, 2, total, head_width), LOW),
        soft=vmem((lines, heads, local, total), F32),
        dkv_all=vmem((2, total, head_width), F32),
        dkv_out=vmem((lines, 2, local, head_width), LOW),
        dkv_in=vmem((lines, 2, local, head_width), LOW),
        part=vmem((4, STREAMS, stream, width), LOW),
        arrived=vmem((lines, 4, STREAMS, peers, sub, width), LOW),
        out_low=vmem((lines, rows, width), LOW),
        grad_low=vmem((lines, rows, width), LOW),
        norm_part=vmem((lines, 8, width), F32),
        norm_all=vmem((lines, 8, width), F32),
        w_first_s=dma((4, 2)),
        w_first_r=dma((lines, 4)),
        w_second_s=dma((lines, 4)),
        w_second_r=dma((lines, 4, 2)),
        w_core_s=dma((lines, 4)),
        w_core_r=dma((lines, 4)),
        w_own=dma((4,)),
        small_s=dma((lines - 1,)),
        small_r=dma((lines,)),
        count_s=dma((lines - 1,)),
        count_r=dma((lines,)),
        ag_s=dma((4, STREAMS, peers)),
        ag_r=dma((4, STREAMS, peers)),
        rs_s=dma((4, STREAMS, peers)),
        rs_r=dma((4, STREAMS, peers)),
        kv_s=dma((lines,)),
        kv_r=dma((lines,)),
        dkv_s=dma((lines,)),
        dkv_r=dma((lines,)),
        rows_s=dma((8, lines, 2)),
        rows_r=dma((8,)),
        share_s=dma((4,)),
        share_r=dma((4,)),
        out_s=dma((lines,)),
        out_r=dma,
        grad_s=dma((lines,)),
        grad_r=dma,
        norm_s=dma((lines,)),
        norm_r=dma,
        ends_s=dma((2 * chips - 1,)),
        ends_r=dma,
    )
    names = tuple(operands) + tuple(outputs) + tuple(scratch)
    results = pl.pallas_call(
        functools.partial(relay_kernel, names),
        out_shape=[jax.ShapeDtypeStruct(shape, kind) for shape, kind in outputs.values()],
        in_specs=[pl.BlockSpec(memory_space=space(name)) for name in operands],
        out_specs=[
            pl.BlockSpec(memory_space=pl.ANY if name in gathered else pltpu.VMEM)
            for name in outputs
        ],
        scratch_shapes=list(scratch.values()),
        compiler_params=pltpu.CompilerParams(
            collective_id=0, has_side_effects=True, vmem_limit_bytes=60 * 2**20
        ),
        name="relay",
    )(*operands.values())
    return dict(zip(outputs, results))


def weights_kernel(names, *refs):
    r = types.SimpleNamespace(**dict(zip(names, refs)))
    step = pl.program_id(0)
    micro_count, rows, buckets, width = r.activations.shape
    chips, units, head_width = r.ends.shape[0] // 2, r.all_act.shape[-1], r.all_mix.shape[-1]

    @pl.when(step == 0)
    def _():
        sums = r.ends[0]
        for other in range(1, 2 * chips):
            sums = sums + r.ends[other]
        singles = (r.ln1_gain, r.ln1_shift, r.ln2_gain, r.ln2_shift, r.b_out, r.b_proj)
        for place, single in enumerate(singles):
            single[...] = sums[place : place + 1]
        for chip in range(chips):
            both = r.ends[chip] + r.ends[chips + chip]
            r.b_fc[:, chip * units : (chip + 1) * units] = both[6:7, :units]
            here = slice(chip * head_width, (chip + 1) * head_width)
            r.b_qv[0:1, here] = both[7:8, :head_width]
            r.b_qv[1:2, here] = both[7:8, width // 2 : width // 2 + head_width]
        for target, source in ((r.activations, r.acts), (r.in_grads, r.grads)):
            for micro in range(micro_count):
                rows_of = [
                    source[micro * buckets + bucket].astype(F32)[:, None, :]
                    for bucket in range(buckets)
                ]
                target[micro] = jnp.concatenate(rows_of, axis=1).astype(LOW)
        for target in (r.w_qkv, r.w_out, r.w_fc, r.w_proj):
            target[...] = jnp.zeros_like(target)

    def rows_of_sequence(ref):
        return ref[0].reshape(2 * chips * rows, ref.shape[-1])

    nrm, nmlp, ups, brn, act, gpre, mix = (
        rows_of_sequence(ref)
        for ref in (r.all_nrm, r.all_nmlp, r.all_ups, r.all_brn, r.all_act, r.all_gpre, r.all_mix)
    )
    r.w_proj[...] += dot_tn(act, ups)
    r.w_fc[...] += dot_tn(nmlp, gpre)
    r.w_out[...] += dot_tn(mix, brn)
    for which in range(3):
        grad = r.all_dqkv[0, :, which].reshape(2 * chips * rows, head_width)
        r.w_qkv[which] += dot_tn(grad, nrm)


def weights_call(relayed, inputs_shape, head_width, units):
    lines = lax.axis_size("section")
    chips = lax.axis_size("tensor")
    width = inputs_shape[-1]
    half = width // 2
    outputs = dict(
        activations=(inputs_shape, LOW),
        in_grads=(inputs_shape, LOW),
        ln1_gain=((1, width), F32),
        ln1_shift=((1, width), F32),
        w_qkv=((3, head_width, half), F32),
        b_qv=((2, width), F32),
        w_out=((head_width, half), F32),
        b_out=((1, width), F32),
        ln2_gain=((1, width), F32),
        ln2_shift=((1, width), F32),
        w_fc=((half, units), F32),
        b_fc=((1, chips * units), F32),
        w_proj=((units, half), F32),
        b_proj=((1, width), F32),
    )

    def spec(array):
        if len(array.shape) < 5:
            return pl.BlockSpec(array.shape, lambda step: (0,) * len(array.shape))
        return pl.BlockSpec(
            (1,) + array.shape[1:], lambda step: (step,) + (0,) * (len(array.shape) - 1)
        )

    def whole(shape):
        return pl.BlockSpec(shape, lambda step: (0,) * len(shape))

    return pl.pallas_call(
        functools.partial(weights_kernel, tuple(relayed) + tuple(outputs)),
        out_shape=[jax.ShapeDtypeStruct(shape, kind) for shape, kind in outputs.values()],
        grid=(lines,),
        in_specs=[spec(array) for array in relayed.values()],
        out_specs=[whole(shape) for shape, _ in outputs.values()],
        compiler_params=pltpu.CompilerParams(vmem_limit_bytes=60 * 2**20),
        name="weight_gradients",
    )(*relayed.values())


def on_line(
    inputs,
    cotangent,
    lengths,
    chosen,
    ln1_gain,
    ln1_shift,
    w_qkv,
    b_qv,
    w_out,
    b_out,
    ln2_gain,
    ln2_shift,
    w_fc,
    b_fc,
    w_proj,
    b_proj,
):
    head_width, units = w_out.shape[1], w_fc.shape[2]
    singles = dict(
        ln1_gain=ln1_gain,
        ln1_shift=ln1_shift,
        ln2_gain=ln2_gain,
        ln2_shift=ln2_shift,
        b_out=b_out,
        b_proj=b_proj,
        b_fc=b_fc,
        b_qv=b_qv[0],
    )
    weights = dict(
        wq_in=jnp.swapaxes(w_qkv[0], 1, 2).reshape(-1, inputs.shape[-1]),
        wo_in=w_out[0],
        wf_in=w_fc[0],
        wp_in=w_proj[0],
    )
    picks = chosen.reshape((-1,) + chosen.shape[-2:])
    relayed = relay_call(inputs, cotangent, lengths, picks, singles, weights)
    results = list(weights_call(relayed, inputs.shape, head_width, units))
    results[4] = jnp.swapaxes(results[4], 1, 2)
    vectors = (2, 3, 7, 8, 9, 11, 13)
    return tuple(
        result if place in vectors else result[None] for place, result in enumerate(results)
    )


def fits_lines(mesh):
    return mesh.shape["section"] == 4 and mesh.shape["seq"] == 2 and mesh.shape["tensor"] == 4


def solution(mesh):
    placed = (
        P(None, ("seq", "tensor"), None, None),
        P(None, ("seq", "tensor"), None, None),
        P(),
        P("section", None, None, "tensor", "seq", None),
        P("section", None),
        P("section", None),
        P("section", None, None, "tensor"),
        P("section", None, "tensor"),
        P("section", "tensor", None),
        P("section", None),
        P("section", None),
        P("section", None),
        P("section", None, "tensor"),
        P("section", "tensor"),
        P("section", "tensor", None),
        P("section", None),
    )
    return jax.shard_map(
        on_line if fits_lines(mesh) else on_device,
        mesh=mesh,
        in_specs=placed,
        out_specs=(
            P("section", None, ("seq", "tensor"), None, None),
            P("section", None, ("seq", "tensor"), None, None),
            P("section", None),
            P("section", None),
            P("section", None, "seq", "tensor"),
            P("section", None, None),
            P("section", "tensor", "seq"),
            P("section", None),
            P("section", None),
            P("section", None),
            P("section", "seq", "tensor"),
            P("section", None),
            P("section", "tensor", "seq"),
            P("section", None),
        ),
        check_vma=False,
    )
```

```python
import functools
import types

import jax
import jax.numpy as jnp
from jax import lax
from jax.experimental import pallas as pl
from jax.experimental.pallas import tpu as pltpu
from jax.sharding import PartitionSpec as P

HDIM = 64
WIN = 64
QB = 64
KSEL = 64


NORM_EPS = 1e-05
MASKED = -1000000000.0


def from_behind(value, axis, steps):
    count = lax.axis_size(axis)
    first, last = (max(0, -steps), min(count, count - steps))
    return lax.ppermute(value, axis, [(source, source + steps) for source in range(first, last)])


def layer_norm(values, gain, shift):
    average = jnp.mean(values, axis=-1, keepdims=True)
    centred = values - average
    variance = jnp.mean(centred * centred, axis=-1, keepdims=True)
    return centred * lax.rsqrt(variance + NORM_EPS) * gain + shift


def gelu_tanh(values):
    return (
        0.5
        * values
        * (1.0 + jnp.tanh(0.7978845608028654 * (values + 0.044715 * values * values * values)))
    )


def gather_rows(row_block):
    return lax.all_gather(row_block, "tensor", axis=0, tiled=True)


def scatter_product(left_rows, weight, formula):
    return lax.psum_scatter(
        jnp.einsum(formula, left_rows, weight, preferred_element_type=jnp.float32).astype(
            jnp.bfloat16
        ),
        "tensor",
        scatter_dimension=0,
        tiled=True,
    ).astype(jnp.float32)


def near_slabs(full_rows, seq_start, seq_first, length_local):
    buckets = full_rows.shape[1]
    heads_local = full_rows.shape[2] // HDIM
    blocks = length_local // QB
    earlier = lax.dynamic_slice_in_dim(full_rows, jnp.maximum(seq_start - WIN, 0), WIN, 0)
    earlier = jnp.where(seq_first, jnp.zeros_like(earlier), earlier)
    local_part = lax.dynamic_slice_in_dim(full_rows, seq_start, length_local, 0)
    segment = jnp.concatenate([earlier, local_part], 0).reshape(
        length_local + WIN, buckets, heads_local, HDIM
    )
    return jnp.concatenate(
        [
            segment[offset_index * QB : offset_index * QB + length_local].reshape(
                blocks, QB, buckets, heads_local, HDIM
            )
            for offset_index in range(WIN // QB + 1)
        ],
        1,
    )


def far_rows(full_rows, flat_index):
    total_rows, buckets, feature_width = full_rows.shape
    heads_local = feature_width // HDIM
    return jnp.take(full_rows.reshape(total_rows * buckets * heads_local, HDIM), flat_index, axis=0)


def key_geometry(chosen_now, seq_start, blocks):
    buckets, heads_local = (chosen_now.shape[0], chosen_now.shape[1])
    bucket_ids = lax.broadcasted_iota(jnp.int32, chosen_now.shape, 0)
    head_ids = lax.broadcasted_iota(jnp.int32, chosen_now.shape, 1)
    flat_index = (chosen_now * buckets + bucket_ids) * heads_local + head_ids
    block_start = seq_start + QB * lax.broadcasted_iota(jnp.int32, (blocks, 1, 1), 0)
    query_ids = lax.broadcasted_iota(jnp.int32, (1, QB, 1), 1)
    key_ids = lax.broadcasted_iota(jnp.int32, (1, 1, WIN + QB), 2)
    distance = query_ids + WIN - key_ids
    near_ok = (distance >= 0) & (distance < WIN) & (block_start + key_ids - WIN >= 0)
    far_ok = chosen_now + WIN <= block_start.reshape(1, 1, blocks, 1)
    near_mask = jnp.broadcast_to(
        near_ok[:, None, None], (blocks, buckets, heads_local, QB, WIN + QB)
    )
    far_mask = jnp.broadcast_to(
        jnp.transpose(far_ok, (2, 0, 1, 3))[:, :, :, None, :],
        (blocks, buckets, heads_local, QB, KSEL),
    )
    return (flat_index, jnp.concatenate([near_mask, far_mask], -1))


def attention_setup(queries, key_rows, value_rows, chosen_now, seq_start, seq_first):
    length_local, buckets, feature_width = queries.shape
    heads_local = feature_width // HDIM
    blocks = length_local // QB
    query_blocks = queries.reshape(blocks, QB, buckets, heads_local, HDIM)
    flat_index, key_mask = key_geometry(chosen_now, seq_start, blocks)
    near_keys = near_slabs(key_rows, seq_start, seq_first, length_local)
    near_values = near_slabs(value_rows, seq_start, seq_first, length_local)
    far_keys = far_rows(key_rows, flat_index)
    far_values = far_rows(value_rows, flat_index)
    near_scores = jnp.einsum(
        "bqnhe,btnhe->bnhqt", query_blocks, near_keys, preferred_element_type=jnp.float32
    )
    far_scores = jnp.einsum(
        "bqnhe,nhbke->bnhqk", query_blocks, far_keys, preferred_element_type=jnp.float32
    )
    scores = jnp.where(
        key_mask, HDIM ** (-0.5) * jnp.concatenate([near_scores, far_scores], -1), MASKED
    )
    return (query_blocks, near_keys, near_values, far_keys, far_values, flat_index, scores)


def attend(queries, key_rows, value_rows, chosen_now, seq_start, seq_first):
    query_blocks, near_keys, near_values, far_keys, far_values, flat_index, scores = (
        attention_setup(queries, key_rows, value_rows, chosen_now, seq_start, seq_first)
    )
    span = WIN + QB
    row_top = jnp.max(scores, -1, keepdims=True)
    exp_terms = jnp.exp(scores - row_top)
    row_total = jnp.sum(exp_terms, -1, keepdims=True)
    softmax_low = (exp_terms / row_total).astype(jnp.bfloat16)
    near_part = jnp.einsum(
        "bnhqt,btnhe->bqnhe",
        softmax_low[..., :span],
        near_values,
        preferred_element_type=jnp.float32,
    )
    far_part = jnp.einsum(
        "bnhqk,nhbke->bqnhe",
        softmax_low[..., span:],
        far_values,
        preferred_element_type=jnp.float32,
    )
    return ((near_part + far_part).reshape(queries.shape), row_top + jnp.log(row_total))


def spread_back(near_grad, far_grad, flat_index, seq_start, seq_first, total_rows):
    blocks, span, buckets, heads_local, head_size = near_grad.shape
    length_local = blocks * QB
    feature_width = heads_local * head_size
    segment = jnp.zeros((length_local + WIN, buckets, heads_local, head_size), jnp.float32)
    for offset_index in range(WIN // QB + 1):
        piece = near_grad[:, offset_index * QB : (offset_index + 1) * QB].reshape(
            length_local, buckets, heads_local, head_size
        )
        segment = segment.at[offset_index * QB : offset_index * QB + length_local].add(piece)
    full_rows = jnp.zeros((total_rows * buckets * heads_local, head_size), jnp.float32)
    full_rows = full_rows.at[flat_index.reshape(-1)].add(far_grad.reshape(-1, head_size))
    full_rows = full_rows.reshape(total_rows, buckets, feature_width)
    local_part = segment[WIN:].reshape(length_local, buckets, feature_width)
    earlier = jnp.where(seq_first, 0.0, segment[:WIN].reshape(WIN, buckets, feature_width))
    full_rows = lax.dynamic_update_slice_in_dim(
        full_rows,
        lax.dynamic_slice_in_dim(full_rows, seq_start, length_local, 0) + local_part,
        seq_start,
        0,
    )
    earlier_start = jnp.maximum(seq_start - WIN, 0)
    full_rows = lax.dynamic_update_slice_in_dim(
        full_rows,
        lax.dynamic_slice_in_dim(full_rows, earlier_start, WIN, 0) + earlier,
        earlier_start,
        0,
    )
    return full_rows


def attend_back(
    queries, key_rows, value_rows, chosen_now, seq_start, seq_first, log_total, grad_mixed
):
    query_blocks, near_keys, near_values, far_keys, far_values, flat_index, scores = (
        attention_setup(queries, key_rows, value_rows, chosen_now, seq_start, seq_first)
    )
    span = WIN + QB
    score_scale = HDIM ** (-0.5)
    grad_blocks = grad_mixed.reshape(query_blocks.shape)
    weights_full = jnp.exp(scores - log_total)
    softmax_low = weights_full.astype(jnp.bfloat16)
    grad_near_weights = jnp.einsum(
        "bqnhe,btnhe->bnhqt", grad_blocks, near_values, preferred_element_type=jnp.float32
    )
    grad_far_weights = jnp.einsum(
        "bqnhe,nhbke->bnhqk", grad_blocks, far_values, preferred_element_type=jnp.float32
    )
    grad_weights = jnp.concatenate([grad_near_weights, grad_far_weights], -1)
    row_dot = jnp.sum(weights_full * grad_weights, -1, keepdims=True)
    grad_scores = (weights_full * (grad_weights - row_dot)).astype(jnp.bfloat16)
    grad_near, grad_far = (grad_scores[..., :span], grad_scores[..., span:])
    grad_queries = score_scale * (
        jnp.einsum("bnhqt,btnhe->bqnhe", grad_near, near_keys, preferred_element_type=jnp.float32)
        + jnp.einsum("bnhqk,nhbke->bqnhe", grad_far, far_keys, preferred_element_type=jnp.float32)
    )
    near_key_grad = score_scale * jnp.einsum(
        "bnhqt,bqnhe->btnhe", grad_near, query_blocks, preferred_element_type=jnp.float32
    )
    far_key_grad = score_scale * jnp.einsum(
        "bnhqk,bqnhe->nhbke", grad_far, query_blocks, preferred_element_type=jnp.float32
    )
    near_value_grad = jnp.einsum(
        "bnhqt,bqnhe->btnhe",
        softmax_low[..., :span],
        grad_blocks,
        preferred_element_type=jnp.float32,
    )
    far_value_grad = jnp.einsum(
        "bnhqk,bqnhe->nhbke",
        softmax_low[..., span:],
        grad_blocks,
        preferred_element_type=jnp.float32,
    )
    total_rows = key_rows.shape[0]
    key_grad = spread_back(
        near_key_grad, far_key_grad, flat_index, seq_start, seq_first, total_rows
    )
    value_grad = spread_back(
        near_value_grad, far_value_grad, flat_index, seq_start, seq_first, total_rows
    )
    return (grad_queries.reshape(queries.shape), key_grad, value_grad)


def forward_pass(hidden, params, chosen_now, query_mask, seq_start, seq_first, finish):
    (
        ln1_gain,
        ln1_shift,
        w_qkv,
        b_qv,
        w_out,
        b_out,
        ln2_gain,
        ln2_shift,
        w_fc,
        b_fc,
        w_proj,
        b_proj,
    ) = params
    hidden_wide = hidden.astype(jnp.float32)
    normed_all = gather_rows(layer_norm(hidden_wide, ln1_gain, ln1_shift).astype(jnp.bfloat16))
    projected = jnp.einsum("pnd,jdc->jpnc", normed_all, w_qkv, preferred_element_type=jnp.float32)
    queries = (projected[0] + b_qv[0]).astype(jnp.bfloat16)
    key_rows, value_rows = (
        lax.all_gather(projected[1].astype(jnp.bfloat16), "seq", axis=0, tiled=True),
        lax.all_gather((projected[2] + b_qv[1]).astype(jnp.bfloat16), "seq", axis=0, tiled=True),
    )
    attended, log_total = attend(queries, key_rows, value_rows, chosen_now, seq_start, seq_first)
    mixed_rows = (attended * query_mask[:, :, None]).astype(jnp.bfloat16)
    middle = hidden_wide + scatter_product(mixed_rows, w_out, "pnc,cd->pnd") + b_out
    normed_mlp = gather_rows(layer_norm(middle, ln2_gain, ln2_shift).astype(jnp.bfloat16))
    pre_active = (
        jnp.einsum("pnd,df->pnf", normed_mlp, w_fc, preferred_element_type=jnp.float32) + b_fc
    )
    active = gelu_tanh(pre_active).astype(jnp.bfloat16)
    if not finish:
        return (
            normed_all,
            queries,
            key_rows,
            value_rows,
            log_total,
            mixed_rows,
            middle,
            normed_mlp,
            pre_active,
            active,
        )
    output = (middle + scatter_product(active, w_proj, "pnf,fd->pnd") + b_proj).astype(jnp.bfloat16)
    return (output, (key_rows, value_rows))


def backward_pass(hidden, upstream, params, chosen_now, query_mask, seq_start, seq_first):
    (
        ln1_gain,
        ln1_shift,
        w_qkv,
        b_qv,
        w_out,
        b_out,
        ln2_gain,
        ln2_shift,
        w_fc,
        b_fc,
        w_proj,
        b_proj,
    ) = params
    (
        normed_all,
        queries,
        key_rows,
        value_rows,
        log_total,
        mixed_rows,
        middle,
        normed_mlp,
        pre_active,
        active,
    ) = forward_pass(hidden, params, chosen_now, query_mask, seq_start, seq_first, False)
    upstream_all = gather_rows(upstream)
    grad_w_proj = jnp.einsum(
        "pnf,pnd->fd", active, upstream_all, preferred_element_type=jnp.float32
    )
    grad_b_proj = jnp.sum(upstream.astype(jnp.float32), axis=(0, 1))
    grad_active = jnp.einsum(
        "pnd,fd->pnf", upstream_all, w_proj, preferred_element_type=jnp.float32
    )
    unused_value, gelu_pull = jax.vjp(gelu_tanh, pre_active)
    grad_pre = gelu_pull(grad_active)[0].astype(jnp.bfloat16)
    grad_w_fc = jnp.einsum("pnd,pnf->df", normed_mlp, grad_pre, preferred_element_type=jnp.float32)
    grad_b_fc = jnp.sum(grad_pre.astype(jnp.float32), axis=(0, 1))
    grad_normed_mlp = scatter_product(grad_pre, w_fc, "pnf,df->pnd")
    unused_norm, second_pull = jax.vjp(layer_norm, middle, ln2_gain, ln2_shift)
    grad_mid_norm, grad_ln2_gain, grad_ln2_shift = second_pull(grad_normed_mlp)
    grad_middle = upstream.astype(jnp.float32) + grad_mid_norm
    grad_branch = grad_middle.astype(jnp.bfloat16)
    grad_b_out = jnp.sum(grad_branch.astype(jnp.float32), axis=(0, 1))
    branch_all = gather_rows(grad_branch)
    grad_w_out = jnp.einsum(
        "pnc,pnd->cd", mixed_rows, branch_all, preferred_element_type=jnp.float32
    )
    grad_mixed = jnp.einsum(
        "pnd,cd->pnc", branch_all, w_out, preferred_element_type=jnp.float32
    ).astype(jnp.bfloat16) * query_mask[:, :, None].astype(jnp.bfloat16)
    grad_queries, key_grad_all, value_grad_all = attend_back(
        queries, key_rows, value_rows, chosen_now, seq_start, seq_first, log_total, grad_mixed
    )
    key_grad, value_grad = (
        lax.psum_scatter(
            key_grad_all.astype(jnp.bfloat16), "seq", scatter_dimension=0, tiled=True
        ).astype(jnp.float32),
        lax.psum_scatter(
            value_grad_all.astype(jnp.bfloat16), "seq", scatter_dimension=0, tiled=True
        ).astype(jnp.float32),
    )
    grad_project = jnp.stack(
        [
            grad_queries.astype(jnp.bfloat16),
            key_grad.astype(jnp.bfloat16),
            value_grad.astype(jnp.bfloat16),
        ],
        2,
    )
    grad_w_qkv = jnp.einsum(
        "pnd,pnjc->jdc", normed_all, grad_project, preferred_element_type=jnp.float32
    )
    grad_b_qv = jnp.sum(grad_project[:, :, 0::2].astype(jnp.float32), axis=(0, 1))
    grad_normed = scatter_product(grad_project, w_qkv, "pnjc,jdc->pnd")
    unused_first, first_pull = jax.vjp(layer_norm, hidden.astype(jnp.float32), ln1_gain, ln1_shift)
    grad_in_norm, grad_ln1_gain, grad_ln1_shift = first_pull(grad_normed)
    grad_hidden = (grad_middle + grad_in_norm).astype(jnp.bfloat16)
    block_grads = (
        grad_ln1_gain,
        grad_ln1_shift,
        grad_w_qkv,
        grad_b_qv,
        grad_w_out,
        grad_b_out,
        grad_ln2_gain,
        grad_ln2_shift,
        grad_w_fc,
        grad_b_fc,
        grad_w_proj,
        grad_b_proj,
    )
    return (grad_hidden, block_grads)


def on_device(
    inputs,
    cotangent,
    lengths,
    chosen,
    ln1_gain,
    ln1_shift,
    w_qkv,
    b_qv,
    w_out,
    b_out,
    ln2_gain,
    ln2_shift,
    w_fc,
    b_fc,
    w_proj,
    b_proj,
):
    params = tuple(
        (
            weight_array[0]
            for weight_array in (
                ln1_gain,
                ln1_shift,
                w_qkv,
                b_qv,
                w_out,
                b_out,
                ln2_gain,
                ln2_shift,
                w_fc,
                b_fc,
                w_proj,
                b_proj,
            )
        )
    )
    section_index = lax.axis_index("section")
    section_count = lax.axis_size("section")
    seq_index = lax.axis_index("seq")
    tensor_index = lax.axis_index("tensor")
    tensor_count = lax.axis_size("tensor")
    micro_count, rows_local, buckets, feature_width = inputs.shape
    length_local = rows_local * tensor_count
    heads_width = w_qkv.shape[-1]
    seq_start = seq_index * length_local
    seq_first = seq_index == 0
    positions = seq_start + lax.broadcasted_iota(jnp.int32, (micro_count, length_local, buckets), 1)
    mask_all = (positions < lengths[:, None, :]).astype(jnp.float32)
    mask_rows = lax.dynamic_slice_in_dim(mask_all, tensor_index * rows_local, rows_local, 1)
    step_count = micro_count + section_count - 1
    chosen_section = chosen[0]
    received = jnp.zeros((rows_local, buckets, feature_width), jnp.bfloat16)
    stored = jnp.zeros((micro_count, rows_local, buckets, feature_width), jnp.bfloat16)
    outputs = jnp.zeros_like(stored)
    for step_index in range(step_count):
        micro_index = step_index - section_index
        running = (micro_index >= 0) & (micro_index < micro_count)
        slot_index = jnp.clip(micro_index, 0, micro_count - 1)
        block_in = jnp.where(
            section_index == 0, lax.dynamic_index_in_dim(inputs, slot_index, 0, False), received
        )
        chosen_now = lax.dynamic_index_in_dim(chosen_section, slot_index, 0, False)
        query_mask = lax.dynamic_index_in_dim(mask_all, slot_index, 0, False)
        result, key_pair = forward_pass(
            block_in, params, chosen_now, query_mask, seq_start, seq_first, True
        )
        stored = jnp.where(
            running, lax.dynamic_update_index_in_dim(stored, block_in, slot_index, 0), stored
        )
        outputs = jnp.where(
            running, lax.dynamic_update_index_in_dim(outputs, result, slot_index, 0), outputs
        )
        received = from_behind(result, "section", 1)
    back_received = jnp.zeros((rows_local, buckets, feature_width), jnp.bfloat16)
    in_grads = jnp.zeros_like(stored)
    totals = None
    for step_index in range(step_count):
        micro_index = step_index - (section_count - 1 - section_index)
        running = (micro_index >= 0) & (micro_index < micro_count)
        slot_index = jnp.clip(micro_index, 0, micro_count - 1)
        chosen_now = lax.dynamic_index_in_dim(chosen_section, slot_index, 0, False)
        query_mask = lax.dynamic_index_in_dim(mask_all, slot_index, 0, False)
        local_mask = lax.dynamic_index_in_dim(mask_rows, slot_index, 0, False)
        top_grad = (
            lax.dynamic_index_in_dim(cotangent, slot_index, 0, False).astype(jnp.float32)
            * local_mask[:, :, None]
        ).astype(jnp.bfloat16)
        upstream = jnp.where(section_index == section_count - 1, top_grad, back_received)
        hidden = lax.dynamic_index_in_dim(stored, slot_index, 0, False)
        grad_hidden, block_grads = backward_pass(
            hidden, upstream, params, chosen_now, query_mask, seq_start, seq_first
        )
        block_grads = tuple(
            (jnp.where(running, grad_part, jnp.zeros_like(grad_part)) for grad_part in block_grads)
        )
        totals = (
            block_grads
            if step_index == 0
            else tuple(
                (total_part + grad_part for total_part, grad_part in zip(totals, block_grads))
            )
        )
        in_grads = jnp.where(
            running, lax.dynamic_update_index_in_dim(in_grads, grad_hidden, slot_index, 0), in_grads
        )
        back_received = from_behind(grad_hidden, "section", -1)
    (
        sum_ln1_gain,
        sum_ln1_shift,
        sum_w_qkv,
        sum_b_qv,
        sum_w_out,
        sum_b_out,
        sum_ln2_gain,
        sum_ln2_shift,
        sum_w_fc,
        sum_b_fc,
        sum_w_proj,
        sum_b_proj,
    ) = totals
    part_qkv, part_out, part_fc, part_proj = (
        lax.psum_scatter(
            sum_w_qkv.astype(jnp.bfloat16), "seq", scatter_dimension=1, tiled=True
        ).astype(jnp.float32),
        lax.psum_scatter(
            sum_w_out.astype(jnp.bfloat16), "seq", scatter_dimension=1, tiled=True
        ).astype(jnp.float32),
        lax.psum_scatter(
            sum_w_fc.astype(jnp.bfloat16), "seq", scatter_dimension=0, tiled=True
        ).astype(jnp.float32),
        lax.psum_scatter(
            sum_w_proj.astype(jnp.bfloat16), "seq", scatter_dimension=1, tiled=True
        ).astype(jnp.float32),
    )
    bias_qv = lax.dynamic_update_slice_in_dim(
        jnp.zeros((2, feature_width), jnp.float32), sum_b_qv, tensor_index * heads_width, 1
    )
    units_local = sum_b_fc.shape[0]
    bias_fc = lax.dynamic_update_slice_in_dim(
        jnp.zeros((units_local * tensor_count,), jnp.float32),
        sum_b_fc,
        tensor_index * units_local,
        0,
    )
    small_sums = lax.psum(
        (
            sum_ln1_gain,
            sum_ln1_shift,
            bias_qv,
            sum_b_out,
            sum_ln2_gain,
            sum_ln2_shift,
            bias_fc,
            sum_b_proj,
        ),
        ("seq", "tensor"),
    )
    return (
        outputs[None],
        in_grads[None],
        small_sums[0][None],
        small_sums[1][None],
        part_qkv[None],
        small_sums[2][None],
        part_out[None],
        small_sums[3][None],
        small_sums[4][None],
        small_sums[5][None],
        part_fc[None],
        small_sums[6][None],
        part_proj[None],
        small_sums[7][None],
    )


STREAMS = 2
NRM, NMLP, UPS, BRN, ACT, GPRE, MIX, DQKV = range(8)
F32 = jnp.float32
LOW = jnp.bfloat16
MESH_ID = pl.DeviceIdType.MESH


def dot_nn(left, right):
    return lax.dot_general(left, right, (((1,), (0,)), ((), ())), preferred_element_type=F32)


def dot_nt(left, right):
    return lax.dot_general(left, right, (((1,), (1,)), ((), ())), preferred_element_type=F32)


def dot_tn(left, right):
    return lax.dot_general(left, right, (((0,), (0,)), ((), ())), preferred_element_type=F32)


def standard(rows):
    centred = rows - jnp.mean(rows, axis=-1, keepdims=True)
    scale = lax.rsqrt(jnp.mean(centred * centred, axis=-1, keepdims=True) + NORM_EPS)
    return centred * scale, scale


def standard_back(grad, xhat, scale):
    inner = jnp.mean(grad * xhat, axis=-1, keepdims=True)
    return scale * (grad - jnp.mean(grad, axis=-1, keepdims=True) - xhat * inner)


def column_sum(rows):
    return jnp.sum(rows.astype(F32), axis=0, keepdims=True)


def relay_kernel(names, *refs):
    r = types.SimpleNamespace(**dict(zip(names, refs)))
    a, c, t = (lax.axis_index(name) for name in ("section", "seq", "tensor"))
    lines = lax.axis_size("section")
    chips = lax.axis_size("tensor")
    rows, buckets, width = r.inputs.shape[1:]
    half_width = width // 2
    local = rows * chips
    total = 2 * local
    sub = rows // STREAMS
    stream_rows = local // STREAMS
    head_width = r.wo_in.shape[0]
    heads = head_width // HDIM
    blocks = local // QB
    units = r.wp_in.shape[0]
    scale = HDIM ** (-0.5)
    streams = range(STREAMS)

    def remote(src, dst, send, recv, **target):
        return pltpu.make_async_remote_copy(
            src_ref=src,
            dst_ref=dst,
            send_sem=send,
            recv_sem=recv,
            device_id=target,
            device_id_type=MESH_ID,
        )

    def drain(ref, sem):
        pltpu.make_async_copy(ref, ref, sem).wait()

    def row_block(index, size):
        return pl.ds(pl.multiple_of(index * size, size), size)

    mine = row_block(t, sub)
    my_half = row_block(c, local)

    barrier = pltpu.get_barrier_semaphore()
    for core in range(2):
        for step in range(1, chips):
            there = {"tensor": (t + step) % chips, "seq": core}
            pl.semaphore_signal(barrier, inc=1, device_id=there, device_id_type=MESH_ID)
        for step in range(1, lines):
            there = {"section": (a + step) % lines, "seq": core}
            pl.semaphore_signal(barrier, inc=1, device_id=there, device_id_type=MESH_ID)
    pl.semaphore_signal(barrier, inc=1, device_id={"seq": 1 - c}, device_id_type=MESH_ID)
    pl.semaphore_wait(barrier, 2 * (chips - 1) + 2 * (lines - 1) + 1)

    def beside(s):
        return s + 1 - 2 * (s % 2)

    def above(s):
        return (s + 2) % 4

    def store(p):
        return (r.wq, r.wo, r.wf, r.wp)[p]

    def source(p):
        return (r.wq_in, r.wo_in, r.wf_in, r.wp_in)[p]

    def height(p):
        return source(p).shape[0]

    def core_half(p, s, core):
        return store(p).at[s, row_block(core, height(p) // 2)]

    def first_hop(p, s, neighbour, which):
        return remote(
            source(p).at[row_block(c, height(p) // 2)],
            core_half(p, s, c),
            r.w_first_s.at[p, which],
            r.w_first_r.at[s, p],
            section=neighbour,
        )

    def second_hop(p, s, which):
        view = store(p).at[s, row_block(2 * c + which, height(p) // 4)]
        return remote(
            view, view, r.w_second_s.at[s, p], r.w_second_r.at[s, p, which], section=3 - s
        )

    def core_hop(p, s, core):
        view = core_half(p, s, core)
        return remote(view, view, r.w_core_s.at[s, p], r.w_core_r.at[s, p], seq=1 - c)

    def own_copy(p):
        return pltpu.make_async_copy(source(p), store(p).at[a], r.w_own.at[p])

    def pass_on(s, p):
        for which, line in enumerate((beside(s), above(s))):

            @pl.when(a == line)
            def _():
                first_hop(p, s, line, which).wait_recv()
                second_hop(p, s, which).start()
                core_hop(p, s, c).start()

    def pass_far(s, p):
        @pl.when(a == 3 - s)
        def _():
            second_hop(p, s, 0).wait_recv()
            second_hop(p, s, 1).wait_recv()
            core_hop(p, s, c).start()

    def need(s, p):
        @pl.when(s == 0)
        def _():
            pass_on(s, p)
            pass_far(s, p)

        @pl.when(a == s)
        def _():
            own_copy(p).wait()

        @pl.when(a != s)
        def _():
            core_hop(p, s, 1 - c).wait_recv()

    def small_copy(step, line, slot):
        return remote(
            r.small_own, r.small.at[slot], r.small_s.at[step], r.small_r.at[slot], section=line
        )

    def count_copy(step, line, slot):
        return remote(
            r.count_own.at[line],
            r.count.at[slot],
            r.count_s.at[step],
            r.count_r.at[slot],
            section=line,
        )

    singles = (r.ln1_gain, r.ln1_shift, r.ln2_gain, r.ln2_shift, r.b_out, r.b_proj)
    for place, single in enumerate(singles):
        r.small_own[place : place + 1] = single[...]
    r.small_own[6:7, :units] = r.b_fc[...]
    r.small_own[7:8, :head_width] = r.b_qv[0:1]
    r.small_own[7:8, half_width : half_width + head_width] = r.b_qv[1:2]
    for step in range(1, lines):
        small_copy(step - 1, (a + step) % lines, a).start()
    for p in range(4):
        for which, line in enumerate((beside(a), above(a))):
            first_hop(p, a, line, which).start()
    for p in range(4):
        own_copy(p).start()
    r.small[a] = r.small_own[...]

    def place_of(index):
        inside = index % local
        stream, left = inside // stream_rows, inside % stream_rows
        return (index // local) * local + (left // sub) * rows + stream * sub + left % sub

    def iota(shape, dimension):
        return lax.broadcasted_iota(jnp.int32, shape, dimension)

    square = jnp.where(iota((KSEL, KSEL), 0) == iota((KSEL, KSEL), 1), 1.0, 0.0).astype(LOW)
    position = place_of(iota((KSEL, total), 1)).astype(F32)
    for pair in range(lines * heads):
        line, head = pair // heads, pair % heads
        columns = dot_nt(square, r.chosen[pair].astype(F32).astype(LOW))
        for block in range(blocks):
            pick = head * blocks + block
            r.count_own[line, pick : pick + 1, :] = jnp.sum(
                jnp.where(columns[:, block : block + 1] == position, 1.0, 0.0),
                axis=0,
                keepdims=True,
            )
    for step in range(1, lines):
        count_copy(step - 1, (a + step) % lines, a).start()
    r.count[a] = r.count_own[a]

    near_chip = t + 1 - 2 * (t % 2)
    over_chip = (t + 2) % 4
    across_chip = 3 - t
    middle_chip = (t == 1) | (t == 2)
    end_chip = (t == 0) | (t == 3)
    ACROSS, OVER, NEAR, PASSED = range(4)

    def gather(buffer, s, kind, j, chip, target, sent_as, comes_as):
        view = buffer.at[s, j, row_block(chip, sub)]
        return remote(
            view,
            view,
            r.ag_s.at[kind, j, sent_as],
            r.ag_r.at[kind, j, comes_as],
            tensor=target,
        )

    def gather_start(buffer, s, kind, j):
        gather(buffer, s, kind, j, t, over_chip, OVER, OVER).start()

        @pl.when(middle_chip)
        def _():
            gather(buffer, s, kind, j, t, across_chip, ACROSS, ACROSS).start()

        gather(buffer, s, kind, j, t, near_chip, NEAR, NEAR).start()

    def gather_wait(buffer, s, kind, j):
        gather(buffer, s, kind, j, over_chip, over_chip, OVER, OVER).wait_recv()

        @pl.when(middle_chip)
        def _():
            gather(buffer, s, kind, j, over_chip, near_chip, PASSED, ACROSS).start()

        gather(buffer, s, kind, j, near_chip, near_chip, NEAR, NEAR).wait_recv()
        gather(buffer, s, kind, j, across_chip, across_chip, ACROSS, ACROSS).wait_recv()

    def gather_sent(buffer, s, kind, j):
        gather(buffer, s, kind, j, t, over_chip, OVER, OVER).wait_send()
        gather(buffer, s, kind, j, t, near_chip, NEAR, NEAR).wait_send()

        @pl.when(middle_chip)
        def _():
            gather(buffer, s, kind, j, t, across_chip, ACROSS, ACROSS).wait_send()
            gather(buffer, s, kind, j, over_chip, near_chip, PASSED, ACROSS).wait_send()

    def scatter(s, kind, j, chip, target, slot):
        return remote(
            r.part.at[kind, j, row_block(chip, sub)],
            r.arrived.at[s, kind, j, slot],
            r.rs_s.at[kind, j, slot],
            r.rs_r.at[kind, j, slot],
            tensor=target,
        )

    def scatter_start(s, kind, j, product):
        r.part[kind, j] = product.astype(LOW)

        @pl.when(end_chip)
        def _():
            scatter(s, kind, j, across_chip, near_chip, PASSED).start()
            scatter(s, kind, j, over_chip, over_chip, OVER).start()

        @pl.when(middle_chip)
        def _():
            scatter(s, kind, j, across_chip, across_chip, ACROSS).start()

        scatter(s, kind, j, near_chip, near_chip, NEAR).start()

    def scatter_sum(s, kind, j):
        @pl.when(middle_chip)
        def _():
            scatter(s, kind, j, across_chip, near_chip, PASSED).wait_recv()
            over = row_block(over_chip, sub)
            joined = r.part[kind, j, over].astype(F32) + r.arrived[s, kind, j, PASSED].astype(F32)
            r.part[kind, j, over] = joined.astype(LOW)
            scatter(s, kind, j, over_chip, over_chip, OVER).start()

        result = r.part[kind, j, mine].astype(F32)
        scatter(s, kind, j, near_chip, near_chip, NEAR).wait_recv()
        result = result + r.arrived[s, kind, j, NEAR].astype(F32)

        @pl.when(middle_chip)
        def _():
            scatter(s, kind, j, across_chip, across_chip, ACROSS).wait_recv()

        across = r.arrived[s, kind, j, ACROSS].astype(F32)
        result = result + jnp.where(middle_chip, across, 0.0)
        scatter(s, kind, j, over_chip, over_chip, OVER).wait_recv()
        return result + r.arrived[s, kind, j, OVER].astype(F32)

    def scatter_sent(s, kind, j):
        scatter(s, kind, j, over_chip, over_chip, OVER).wait_send()
        scatter(s, kind, j, near_chip, near_chip, NEAR).wait_send()

        @pl.when(end_chip)
        def _():
            scatter(s, kind, j, across_chip, near_chip, PASSED).wait_send()

        @pl.when(middle_chip)
        def _():
            scatter(s, kind, j, across_chip, across_chip, ACROSS).wait_send()

    own_rows = (r.nrm, r.nmlp, r.ups, r.brn, r.act, r.gpre, r.mix, r.dqkv)
    all_rows = (
        r.all_nrm,
        r.all_nmlp,
        r.all_ups,
        r.all_brn,
        r.all_act,
        r.all_gpre,
        r.all_mix,
        r.all_dqkv,
    )

    def rows_copy(index, s, same, stays=False):
        core = c if same else 1 - c
        src = own_rows[index].at[s]
        dst = all_rows[index].at[a, c]
        if index <= BRN:
            src = src.at[:, :, row_block(core, half_width)]
        recv = r.rows_r.at[index]
        if stays:
            return pltpu.make_async_copy(src, dst, recv)
        if same:
            return remote(src, dst, r.rows_s.at[index, s, 0], recv, section=s)
        return remote(src, dst, r.rows_s.at[index, s, 1], recv, section=s, seq=1 - c)

    def rows_start(index, s):
        @pl.when(a == s)
        def _():
            rows_copy(index, s, True, True).start()

        @pl.when(a != s)
        def _():
            rows_copy(index, s, True).start()

        if index <= BRN:
            rows_copy(index, s, False).start()

    def rows_sent(index, s):
        @pl.when(a != s)
        def _():
            rows_copy(index, s, True).wait_send()

        if index <= BRN:
            rows_copy(index, s, False).wait_send()

    def share_copy(index, core):
        view = all_rows[index].at[:, core]
        return remote(view, view, r.share_s.at[index - ACT], r.share_r.at[index - ACT], seq=1 - c)

    def share(index):
        drain(all_rows[index].at[:, c], r.rows_r.at[index])
        share_copy(index, c).start()

    def home_copy(src, dst, send, recv, s):
        return remote(src.at[s], dst.at[a], send.at[s], recv, section=s)

    def home_start(src, dst, send, recv, s):
        @pl.when(a == s)
        def _():
            pltpu.make_async_copy(src.at[s], dst.at[a], recv).start()

        @pl.when(a != s)
        def _():
            home_copy(src, dst, send, recv, s).start()

    def home_sent(*what):
        @pl.when(a != what[-1])
        def _():
            home_copy(*what).wait_send()

    out_home = (r.out_low, r.acts, r.out_s, r.out_r)
    grad_home = (r.grad_low, r.grads, r.grad_s, r.grad_r)
    norm_home = (r.norm_part, r.norm_all, r.norm_s, r.norm_r)

    length = r.lengths[a // buckets, a % buckets]
    query = place_of(c * local + iota((local, total), 0))
    key = place_of(iota((local, total), 1))
    near = jnp.where((query >= key) & (query - key < WIN), 1.0, 0.0)
    key_row = place_of(iota((1, total), 1))
    block_of = place_of(iota((local, total), 0)) // QB
    first_block = jnp.where(block_of == 0, 1.0, 0.0)

    def row_mask(place):
        return jnp.where(place < length, 1.0, 0.0)

    def multiplicity(s, head):
        times = near
        for block in range(blocks):
            pick = head * blocks + block
            limit = (c * blocks + block) * QB - WIN
            counted = jnp.where(key_row <= limit, r.count[s, pick : pick + 1, :], 0.0)
            times = times + jnp.where(block_of == block, counted, 0.0)
        return times

    def head_cols(head):
        return slice(head * HDIM, (head + 1) * HDIM)

    def kv_copy(s, core):
        view = r.kv.at[s, :, row_block(core, local)]
        return remote(view, view, r.kv_s.at[s], r.kv_r.at[s], seq=1 - c)

    def dkv_copy(s):
        return remote(r.dkv_out.at[s], r.dkv_in.at[s], r.dkv_s.at[s], r.dkv_r.at[s], seq=1 - c)

    def flat(array):
        return array.reshape(local, array.shape[-1])

    def own_sequence(ref):
        both = ref[a // buckets].astype(F32)
        picked = both[:, 0, :]
        for bucket in range(1, buckets):
            picked = jnp.where(a % buckets == bucket, both[:, bucket, :], picked)
        return picked

    def part_rows(j):
        return slice(j * sub, (j + 1) * sub)

    r.hidden[...] = own_sequence(r.inputs)
    own_place = c * local + t * rows + iota((rows, 1), 0)
    r.upstream[...] = (own_sequence(r.cotangent) * row_mask(own_place)).astype(LOW)
    r.norm_part[...] = jnp.zeros_like(r.norm_part)

    def enter(s, j):
        xhat, inverse = standard(r.hidden[part_rows(j)])
        r.xhat1[s, j] = xhat
        r.inv1[s, j] = jnp.broadcast_to(inverse, (sub, 128))
        r.nrm[s, j, mine] = (xhat * r.small[s, 0:1] + r.small[s, 1:2]).astype(LOW)
        gather_start(r.nrm, s, 0, j)

    def project(s, j):
        gather_wait(r.nrm, s, 0, j)
        normed = r.nrm[s, j]
        place = row_block(c * STREAMS + j, stream_rows)
        bias_v = r.small[s, 7:8, half_width : half_width + head_width]
        key_rows = dot_nt(normed, r.wq[s, head_width : 2 * head_width])
        value_rows = dot_nt(normed, r.wq[s, 2 * head_width : 3 * head_width]) + bias_v
        r.kv[s, 0, place] = key_rows.astype(LOW)
        r.kv[s, 1, place] = value_rows.astype(LOW)
        gather_sent(r.nrm, s, 0, j)

    def ask(s, j):
        queries = dot_nt(r.nrm[s, j], r.wq[s, 0:head_width]) + r.small[s, 7:8, :head_width]
        r.qry[s, j] = queries.astype(LOW)

    def attend_line(s):
        mixed = []
        queries = flat(r.qry[s])
        for head in range(heads):
            times = multiplicity(s, head)
            scores = scale * dot_nt(queries[:, head_cols(head)], r.kv[s, 0, :, head_cols(head)])
            scores = jnp.where(times > 0.0, scores, MASKED)
            top = jnp.max(scores, axis=-1, keepdims=True)
            terms = times * jnp.exp(scores - top)
            weights = terms / jnp.sum(terms, axis=-1, keepdims=True)
            r.soft[s, head] = weights
            mixed.append(dot_nn(weights.astype(LOW), r.kv[s, 1, :, head_cols(head)]))
        mask = row_mask(place_of(c * local + iota((local, 1), 0)))
        mixed = (jnp.concatenate(mixed, axis=-1) * mask).astype(LOW)
        r.mix[s] = mixed.reshape(r.mix.shape[1:])

    def leave_attention(s, j):
        scatter_start(s, 0, j, dot_nn(r.mix[s, j], r.wo[s]))

    def between(s, j):
        middle = r.hidden[part_rows(j)] + scatter_sum(s, 0, j) + r.small[s, 4:5]
        r.middle[part_rows(j)] = middle
        scatter_sent(s, 0, j)
        xhat, inverse = standard(middle)
        r.xhat2[s, j] = xhat
        r.inv2[s, j] = jnp.broadcast_to(inverse, (sub, 128))
        r.nmlp[s, j, mine] = (xhat * r.small[s, 2:3] + r.small[s, 3:4]).astype(LOW)
        gather_start(r.nmlp, s, 1, j)

    def feed(s, j):
        gather_wait(r.nmlp, s, 1, j)
        before = dot_nn(r.nmlp[s, j], r.wf[s]) + r.small[s, 6:7, :units]
        bend = jnp.tanh(0.7978845608028654 * (before + 0.044715 * before * before * before))
        r.act[s, j] = (0.5 * before * (1.0 + bend)).astype(LOW)
        r.slope[s, j] = 0.5 * (1.0 + bend) + 0.5 * before * (1.0 - bend * bend) * (
            0.7978845608028654 * (1.0 + 3 * 0.044715 * before * before)
        )

        gather_sent(r.nmlp, s, 1, j)

    def leave_feed(s, j):
        scatter_start(s, 1, j, dot_nn(r.act[s, j], r.wp[s]))

    def finish(s, j):
        result = r.middle[part_rows(j)] + scatter_sum(s, 1, j) + r.small[s, 5:6]
        r.out_low[s, part_rows(j)] = result.astype(LOW)
        r.hidden[part_rows(j)] = result.astype(LOW).astype(F32)
        scatter_sent(s, 1, j)

    def small_ready(s):
        @pl.when(a != s)
        def _():
            small_copy(0, a, s).wait_recv()

    small_ready(0)
    for j in streams:
        enter(0, j)

    def forward(s, _):
        need(s, 0)
        for j in streams:
            project(s, j)
        kv_copy(s, c).start()
        for j in streams:
            ask(s, j)
        rows_start(NRM, s)

        @pl.when(a != s)
        def _():
            count_copy(0, a, s).wait_recv()

        kv_copy(s, 1 - c).wait_recv()
        attend_line(s)
        need(s, 1)
        for j in streams:
            leave_attention(s, j)
        rows_start(MIX, s)
        for j in streams:
            between(s, j)
        need(s, 2)
        for j in streams:
            feed(s, j)
            if j == 0:
                need(s, 3)
            leave_feed(s, j)
        rows_start(NMLP, s)
        rows_start(ACT, s)

        @pl.when(s + 1 < lines)
        def _():
            small_ready(s + 1)

        for j in streams:
            finish(s, j)

            @pl.when(s + 1 < lines)
            def _():
                enter(s + 1, j)

        home_start(*out_home, s)

        @pl.when(s == 0)
        def _():
            for later in range(1, lines):
                for p in range(4):
                    pass_on(later, p)

        @pl.when(s + 1 < lines)
        def _():
            for p in range(4):
                pass_far(s + 1, p)

        return 0

    lax.fori_loop(0, lines, forward, 0)

    def turn(s, j):
        upstream = r.upstream[part_rows(j)]
        r.ups[s, j, mine] = upstream
        gather_start(r.ups, s, 2, j)
        r.norm_part[s, 5:6] += column_sum(upstream)

    def feed_back(s, j):
        gather_wait(r.ups, s, 2, j)
        grad_pre = (dot_nt(r.ups[s, j], r.wp[s]) * r.slope[s, j]).astype(LOW)
        r.gpre[s, j] = grad_pre
        scatter_start(s, 2, j, dot_nt(grad_pre, r.wf[s]))
        r.norm_part[s, 6:7, :units] += column_sum(grad_pre)
        gather_sent(r.ups, s, 2, j)

    def between_back(s, j):
        grad = scatter_sum(s, 2, j)
        xhat = r.xhat2[s, j]
        upstream = r.upstream[part_rows(j)].astype(F32)
        grad_middle = upstream + standard_back(
            grad * r.small[s, 2:3], xhat, r.inv2[s, j, :, 0:1]
        )
        r.middle[part_rows(j)] = grad_middle
        branch = grad_middle.astype(LOW)
        r.brn[s, j, mine] = branch
        gather_start(r.brn, s, 3, j)
        r.norm_part[s, 2:3] += column_sum(grad * xhat)
        r.norm_part[s, 3:4] += column_sum(grad)
        r.norm_part[s, 4:5] += column_sum(branch)
        scatter_sent(s, 2, j)

    def mixed_back(s, j):
        gather_wait(r.brn, s, 3, j)
        place = place_of(c * local + j * stream_rows + iota((stream_rows, 1), 0))
        r.gmix[j] = (dot_nt(r.brn[s, j], r.wo[s]) * row_mask(place)).astype(LOW)
        gather_sent(r.brn, s, 3, j)

    def attend_line_back(s):
        grad_q, grad_k, grad_v = [], [], []
        grad_mixed = flat(r.gmix[...])
        queries = flat(r.qry[s])
        for head in range(heads):
            cols = head_cols(head)
            weights = r.soft[s, head]
            grad_head = grad_mixed[:, cols]
            grad_weights = dot_nt(grad_head, r.kv[s, 1, :, cols])
            inner = jnp.sum(weights * grad_weights, axis=-1, keepdims=True)
            grad_scores = (weights * (grad_weights - inner)).astype(LOW)
            grad_k.append(scale * dot_tn(grad_scores, queries[:, cols]))
            grad_v.append(dot_tn(weights.astype(LOW), grad_head))
            grad_q.append(scale * dot_nn(grad_scores, r.kv[s, 0, :, cols]))
        r.dkv_all[0] = jnp.concatenate(grad_k, axis=-1)
        r.dkv_all[1] = jnp.concatenate(grad_v, axis=-1)
        r.dkv_out[s] = r.dkv_all[:, row_block(1 - c, local)].astype(LOW)
        dkv_copy(s).start()
        grad_q = jnp.concatenate(grad_q, axis=-1).astype(LOW)
        r.dqkv[s, 0] = grad_q.reshape(r.dqkv.shape[2:])
        r.norm_part[s, 7:8, :head_width] = column_sum(grad_q)
        dkv_copy(s).wait_recv()
        for which in range(2):
            joined = r.dkv_all[which, my_half] + r.dkv_in[s, which].astype(F32)
            joined = joined.astype(LOW)
            r.dqkv[s, 1 + which] = joined.reshape(r.dqkv.shape[2:])
            if which == 1:
                r.norm_part[s, 7:8, half_width : half_width + head_width] = column_sum(joined)

    def leave_back(s, j):
        product = dot_nn(r.dqkv[s, 0, j], r.wq[s, 0:head_width])
        for which in range(1, 3):
            weight = r.wq[s, which * head_width : (which + 1) * head_width]
            product = product + dot_nn(r.dqkv[s, which, j], weight)
        scatter_start(s, 3, j, product)

    def finish_back(s, j):
        grad = scatter_sum(s, 3, j)
        xhat = r.xhat1[s, j]
        result = r.middle[part_rows(j)] + standard_back(
            grad * r.small[s, 0:1], xhat, r.inv1[s, j, :, 0:1]
        )
        r.upstream[part_rows(j)] = result.astype(LOW)
        r.grad_low[s, part_rows(j)] = result.astype(LOW)
        r.norm_part[s, 0:1] += column_sum(grad * xhat)
        r.norm_part[s, 1:2] += column_sum(grad)
        scatter_sent(s, 3, j)

    for j in streams:
        turn(lines - 1, j)

    def backward(index, _):
        s = lines - 1 - index
        for j in streams:
            feed_back(s, j)
        rows_start(UPS, s)
        rows_start(GPRE, s)

        @pl.when(index == 1)
        def _():
            share(ACT)
            share(MIX)

        for j in streams:
            between_back(s, j)
        for j in streams:
            mixed_back(s, j)
        rows_start(BRN, s)
        attend_line_back(s)
        for j in streams:
            leave_back(s, j)
        rows_start(DQKV, s)
        for j in streams:
            finish_back(s, j)

            @pl.when(s > 0)
            def _():
                turn(s - 1, j)

        home_start(*norm_home, s)
        home_start(*grad_home, s)
        return 0

    lax.fori_loop(0, lines, backward, 0)

    share(GPRE)
    share(DQKV)

    drain(r.norm_all, r.norm_r)
    slot = c * chips + t
    norm_sum = r.norm_all[0]
    for line in range(1, lines):
        norm_sum = norm_sum + r.norm_all[line]
    r.ends[slot] = norm_sum

    def ends_copy(step):
        core, chip = step // chips, step % chips
        view = r.ends.at[slot]
        return remote(
            view,
            view,
            r.ends_s.at[step - 1],
            r.ends_r,
            seq=(c + core) % 2,
            tensor=(t + chip) % chips,
        )

    for step in range(1, 2 * chips):
        ends_copy(step).start()

    for index in range(ACT):
        drain(all_rows[index], r.rows_r.at[index])
    for index in range(ACT, 8):
        share_copy(index, 1 - c).wait_recv()
        share_copy(index, c).wait_send()
    drain(r.acts, r.out_r)
    drain(r.grads, r.grad_r)
    drain(r.ends.at[0 : 2 * chips - 1], r.ends_r)
    for step in range(1, 2 * chips):
        ends_copy(step).wait_send()
    for step in range(1, lines):
        small_copy(step - 1, (a + step) % lines, a).wait_send()
        count_copy(step - 1, (a + step) % lines, a).wait_send()
    for p in range(4):
        for which, line in enumerate((beside(a), above(a))):
            first_hop(p, a, line, which).wait_send()

    def sent(s, _):
        home_sent(*out_home, s)
        home_sent(*grad_home, s)
        home_sent(*norm_home, s)
        kv_copy(s, c).wait_send()
        dkv_copy(s).wait_send()
        for index in range(8):
            rows_sent(index, s)
        for p in range(4):

            @pl.when((a == beside(s)) | (a == above(s)))
            def _():
                second_hop(p, s, 0).wait_send()

            @pl.when(a != s)
            def _():
                core_hop(p, s, c).wait_send()

        return 0

    lax.fori_loop(0, lines, sent, 0)


def relay_call(inputs, cotangent, lengths, chosen, singles, weights):
    lines = lax.axis_size("section")
    chips = lax.axis_size("tensor")
    rows, buckets, width = inputs.shape[1:]
    local, total, half = rows * chips, 2 * rows * chips, width // 2
    head_width, units = weights["wo_in"].shape[0], weights["wp_in"].shape[0]
    heads = head_width // HDIM
    sub, stream = rows // STREAMS, local // STREAMS
    vmem, dma = pltpu.VMEM, pltpu.SemaphoreType.DMA
    operands = dict(
        inputs=inputs,
        cotangent=cotangent,
        lengths=lengths,
        chosen=chosen,
        **singles,
        **weights,
    )

    def space(name):
        if name in weights:
            return pl.ANY
        return pltpu.SMEM if operands[name] is lengths else pltpu.VMEM

    sums = dict(
        acts=((lines, rows, width), LOW),
        grads=((lines, rows, width), LOW),
        ends=((2 * chips, 8, width), F32),
    )
    gathered = dict(
        all_nrm=((lines, 2, STREAMS, stream, half), LOW),
        all_nmlp=((lines, 2, STREAMS, stream, half), LOW),
        all_ups=((lines, 2, STREAMS, stream, half), LOW),
        all_brn=((lines, 2, STREAMS, stream, half), LOW),
        all_act=((lines, 2, STREAMS, stream, units), LOW),
        all_gpre=((lines, 2, STREAMS, stream, units), LOW),
        all_mix=((lines, 2, STREAMS, stream, head_width), LOW),
        all_dqkv=((lines, 2, 3, STREAMS, stream, head_width), LOW),
    )
    outputs = dict(**sums, **gathered)
    scratch = dict(
        wq=vmem((lines,) + weights["wq_in"].shape, LOW),
        wo=vmem((lines,) + weights["wo_in"].shape, LOW),
        wf=vmem((lines,) + weights["wf_in"].shape, LOW),
        wp=vmem((lines,) + weights["wp_in"].shape, LOW),
        small_own=vmem((8, width), F32),
        small=vmem((lines, 8, width), F32),
        count_own=vmem((lines, 8, total), F32),
        count=vmem((lines, 8, total), F32),
        hidden=vmem((rows, width), F32),
        middle=vmem((rows, width), F32),
        upstream=vmem((rows, width), LOW),
        xhat1=vmem((lines, STREAMS, sub, width), F32),
        inv1=vmem((lines, STREAMS, sub, 128), F32),
        xhat2=vmem((lines, STREAMS, sub, width), F32),
        inv2=vmem((lines, STREAMS, sub, 128), F32),
        nrm=vmem((lines, STREAMS, stream, width), LOW),
        nmlp=vmem((lines, STREAMS, stream, width), LOW),
        ups=vmem((lines, STREAMS, stream, width), LOW),
        brn=vmem((lines, STREAMS, stream, width), LOW),
        act=vmem((lines, STREAMS, stream, units), LOW),
        gpre=vmem((lines, STREAMS, stream, units), LOW),
        slope=vmem((lines, STREAMS, stream, units), F32),
        mix=vmem((lines, STREAMS, stream, head_width), LOW),
        qry=vmem((lines, STREAMS, stream, head_width), LOW),
        gmix=vmem((STREAMS, stream, head_width), LOW),
        dqkv=vmem((lines, 3, STREAMS, stream, head_width), LOW),
        kv=vmem((lines, 2, total, head_width), LOW),
        soft=vmem((lines, heads, local, total), F32),
        dkv_all=vmem((2, total, head_width), F32),
        dkv_out=vmem((lines, 2, local, head_width), LOW),
        dkv_in=vmem((lines, 2, local, head_width), LOW),
        part=vmem((4, STREAMS, stream, width), LOW),
        arrived=vmem((lines, 4, STREAMS, 4, sub, width), LOW),
        out_low=vmem((lines, rows, width), LOW),
        grad_low=vmem((lines, rows, width), LOW),
        norm_part=vmem((lines, 8, width), F32),
        norm_all=vmem((lines, 8, width), F32),
        w_first_s=dma((4, 2)),
        w_first_r=dma((lines, 4)),
        w_second_s=dma((lines, 4)),
        w_second_r=dma((lines, 4, 2)),
        w_core_s=dma((lines, 4)),
        w_core_r=dma((lines, 4)),
        w_own=dma((4,)),
        small_s=dma((lines - 1,)),
        small_r=dma((lines,)),
        count_s=dma((lines - 1,)),
        count_r=dma((lines,)),
        ag_s=dma((4, STREAMS, 4)),
        ag_r=dma((4, STREAMS, 4)),
        rs_s=dma((4, STREAMS, 4)),
        rs_r=dma((4, STREAMS, 4)),
        kv_s=dma((lines,)),
        kv_r=dma((lines,)),
        dkv_s=dma((lines,)),
        dkv_r=dma((lines,)),
        rows_s=dma((8, lines, 2)),
        rows_r=dma((8,)),
        share_s=dma((4,)),
        share_r=dma((4,)),
        out_s=dma((lines,)),
        out_r=dma,
        grad_s=dma((lines,)),
        grad_r=dma,
        norm_s=dma((lines,)),
        norm_r=dma,
        ends_s=dma((2 * chips - 1,)),
        ends_r=dma,
    )
    names = tuple(operands) + tuple(outputs) + tuple(scratch)
    results = pl.pallas_call(
        functools.partial(relay_kernel, names),
        out_shape=[jax.ShapeDtypeStruct(shape, kind) for shape, kind in outputs.values()],
        in_specs=[pl.BlockSpec(memory_space=space(name)) for name in operands],
        out_specs=[
            pl.BlockSpec(memory_space=pl.ANY if name in gathered else pltpu.VMEM)
            for name in outputs
        ],
        scratch_shapes=list(scratch.values()),
        compiler_params=pltpu.CompilerParams(
            collective_id=0, has_side_effects=True, vmem_limit_bytes=60 * 2**20
        ),
        name="relay",
    )(*operands.values())
    return dict(zip(outputs, results))


def weights_kernel(names, *refs):
    r = types.SimpleNamespace(**dict(zip(names, refs)))
    step = pl.program_id(0)
    micro_count, rows, buckets, width = r.activations.shape
    chips, units, head_width = r.ends.shape[0] // 2, r.all_act.shape[-1], r.all_mix.shape[-1]

    @pl.when(step == 0)
    def _():
        sums = r.ends[0]
        for other in range(1, 2 * chips):
            sums = sums + r.ends[other]
        singles = (r.ln1_gain, r.ln1_shift, r.ln2_gain, r.ln2_shift, r.b_out, r.b_proj)
        for place, single in enumerate(singles):
            single[...] = sums[place : place + 1]
        for chip in range(chips):
            both = r.ends[chip] + r.ends[chips + chip]
            r.b_fc[:, chip * units : (chip + 1) * units] = both[6:7, :units]
            here = slice(chip * head_width, (chip + 1) * head_width)
            r.b_qv[0:1, here] = both[7:8, :head_width]
            r.b_qv[1:2, here] = both[7:8, width // 2 : width // 2 + head_width]
        for target, source in ((r.activations, r.acts), (r.in_grads, r.grads)):
            for micro in range(micro_count):
                rows_of = [
                    source[micro * buckets + bucket].astype(F32)[:, None, :]
                    for bucket in range(buckets)
                ]
                target[micro] = jnp.concatenate(rows_of, axis=1).astype(LOW)
        for target in (r.w_qkv, r.w_out, r.w_fc, r.w_proj):
            target[...] = jnp.zeros_like(target)

    def rows_of_sequence(ref):
        return ref[0].reshape(2 * chips * rows, ref.shape[-1])

    nrm, nmlp, ups, brn, act, gpre, mix = (
        rows_of_sequence(ref)
        for ref in (r.all_nrm, r.all_nmlp, r.all_ups, r.all_brn, r.all_act, r.all_gpre, r.all_mix)
    )
    r.w_proj[...] += dot_tn(act, ups)
    r.w_fc[...] += dot_tn(nmlp, gpre)
    r.w_out[...] += dot_tn(mix, brn)
    for which in range(3):
        grad = r.all_dqkv[0, :, which].reshape(2 * chips * rows, head_width)
        r.w_qkv[which] += dot_tn(grad, nrm)


def weights_call(relayed, inputs_shape, head_width, units):
    lines = lax.axis_size("section")
    chips = lax.axis_size("tensor")
    width = inputs_shape[-1]
    half = width // 2
    outputs = dict(
        activations=(inputs_shape, LOW),
        in_grads=(inputs_shape, LOW),
        ln1_gain=((1, width), F32),
        ln1_shift=((1, width), F32),
        w_qkv=((3, head_width, half), F32),
        b_qv=((2, width), F32),
        w_out=((head_width, half), F32),
        b_out=((1, width), F32),
        ln2_gain=((1, width), F32),
        ln2_shift=((1, width), F32),
        w_fc=((half, units), F32),
        b_fc=((1, chips * units), F32),
        w_proj=((units, half), F32),
        b_proj=((1, width), F32),
    )

    def spec(array):
        if len(array.shape) < 5:
            return pl.BlockSpec(array.shape, lambda step: (0,) * len(array.shape))
        return pl.BlockSpec(
            (1,) + array.shape[1:], lambda step: (step,) + (0,) * (len(array.shape) - 1)
        )

    def whole(shape):
        return pl.BlockSpec(shape, lambda step: (0,) * len(shape))

    return pl.pallas_call(
        functools.partial(weights_kernel, tuple(relayed) + tuple(outputs)),
        out_shape=[jax.ShapeDtypeStruct(shape, kind) for shape, kind in outputs.values()],
        grid=(lines,),
        in_specs=[spec(array) for array in relayed.values()],
        out_specs=[whole(shape) for shape, _ in outputs.values()],
        compiler_params=pltpu.CompilerParams(vmem_limit_bytes=60 * 2**20),
        name="weight_gradients",
    )(*relayed.values())


def on_line(
    inputs,
    cotangent,
    lengths,
    chosen,
    ln1_gain,
    ln1_shift,
    w_qkv,
    b_qv,
    w_out,
    b_out,
    ln2_gain,
    ln2_shift,
    w_fc,
    b_fc,
    w_proj,
    b_proj,
):
    head_width, units = w_out.shape[1], w_fc.shape[2]
    singles = dict(
        ln1_gain=ln1_gain,
        ln1_shift=ln1_shift,
        ln2_gain=ln2_gain,
        ln2_shift=ln2_shift,
        b_out=b_out,
        b_proj=b_proj,
        b_fc=b_fc,
        b_qv=b_qv[0],
    )
    weights = dict(
        wq_in=jnp.swapaxes(w_qkv[0], 1, 2).reshape(-1, inputs.shape[-1]),
        wo_in=w_out[0],
        wf_in=w_fc[0],
        wp_in=w_proj[0],
    )
    picks = chosen.reshape((-1,) + chosen.shape[-2:])
    relayed = relay_call(inputs, cotangent, lengths, picks, singles, weights)
    results = list(weights_call(relayed, inputs.shape, head_width, units))
    results[4] = jnp.swapaxes(results[4], 1, 2)
    vectors = (2, 3, 7, 8, 9, 11, 13)
    return tuple(
        result if place in vectors else result[None] for place, result in enumerate(results)
    )


def fits_lines(mesh):
    return mesh.shape["section"] == 4 and mesh.shape["seq"] == 2 and mesh.shape["tensor"] == 4


def solution(mesh):
    placed = (
        P(None, ("seq", "tensor"), None, None),
        P(None, ("seq", "tensor"), None, None),
        P(),
        P("section", None, None, "tensor", "seq", None),
        P("section", None),
        P("section", None),
        P("section", None, None, "tensor"),
        P("section", None, "tensor"),
        P("section", "tensor", None),
        P("section", None),
        P("section", None),
        P("section", None),
        P("section", None, "tensor"),
        P("section", "tensor"),
        P("section", "tensor", None),
        P("section", None),
    )
    return jax.shard_map(
        on_line if fits_lines(mesh) else on_device,
        mesh=mesh,
        in_specs=placed,
        out_specs=(
            P("section", None, ("seq", "tensor"), None, None),
            P("section", None, ("seq", "tensor"), None, None),
            P("section", None),
            P("section", None),
            P("section", None, "seq", "tensor"),
            P("section", None, None),
            P("section", "tensor", "seq"),
            P("section", None),
            P("section", None),
            P("section", None),
            P("section", "seq", "tensor"),
            P("section", None),
            P("section", "tensor", "seq"),
            P("section", None),
        ),
        check_vma=False,
    )
```

```python
import functools
import types

import jax
import jax.numpy as jnp
from jax import lax
from jax.experimental import pallas as pl
from jax.experimental.pallas import tpu as pltpu
from jax.sharding import PartitionSpec as P

HDIM = 64
WIN = 64
QB = 64
KSEL = 64


NORM_EPS = 1e-05
MASKED = -1000000000.0


def from_behind(value, axis, steps):
    count = lax.axis_size(axis)
    first, last = (max(0, -steps), min(count, count - steps))
    return lax.ppermute(value, axis, [(source, source + steps) for source in range(first, last)])


def layer_norm(values, gain, shift):
    average = jnp.mean(values, axis=-1, keepdims=True)
    centred = values - average
    variance = jnp.mean(centred * centred, axis=-1, keepdims=True)
    return centred * lax.rsqrt(variance + NORM_EPS) * gain + shift


def gelu_tanh(values):
    return (
        0.5
        * values
        * (1.0 + jnp.tanh(0.7978845608028654 * (values + 0.044715 * values * values * values)))
    )


def gather_rows(row_block):
    return lax.all_gather(row_block, "tensor", axis=0, tiled=True)


def scatter_product(left_rows, weight, formula):
    return lax.psum_scatter(
        jnp.einsum(formula, left_rows, weight, preferred_element_type=jnp.float32).astype(
            jnp.bfloat16
        ),
        "tensor",
        scatter_dimension=0,
        tiled=True,
    ).astype(jnp.float32)


def near_slabs(full_rows, seq_start, seq_first, length_local):
    buckets = full_rows.shape[1]
    heads_local = full_rows.shape[2] // HDIM
    blocks = length_local // QB
    earlier = lax.dynamic_slice_in_dim(full_rows, jnp.maximum(seq_start - WIN, 0), WIN, 0)
    earlier = jnp.where(seq_first, jnp.zeros_like(earlier), earlier)
    local_part = lax.dynamic_slice_in_dim(full_rows, seq_start, length_local, 0)
    segment = jnp.concatenate([earlier, local_part], 0).reshape(
        length_local + WIN, buckets, heads_local, HDIM
    )
    return jnp.concatenate(
        [
            segment[offset_index * QB : offset_index * QB + length_local].reshape(
                blocks, QB, buckets, heads_local, HDIM
            )
            for offset_index in range(WIN // QB + 1)
        ],
        1,
    )


def far_rows(full_rows, flat_index):
    total_rows, buckets, feature_width = full_rows.shape
    heads_local = feature_width // HDIM
    return jnp.take(full_rows.reshape(total_rows * buckets * heads_local, HDIM), flat_index, axis=0)


def key_geometry(chosen_now, seq_start, blocks):
    buckets, heads_local = (chosen_now.shape[0], chosen_now.shape[1])
    bucket_ids = lax.broadcasted_iota(jnp.int32, chosen_now.shape, 0)
    head_ids = lax.broadcasted_iota(jnp.int32, chosen_now.shape, 1)
    flat_index = (chosen_now * buckets + bucket_ids) * heads_local + head_ids
    block_start = seq_start + QB * lax.broadcasted_iota(jnp.int32, (blocks, 1, 1), 0)
    query_ids = lax.broadcasted_iota(jnp.int32, (1, QB, 1), 1)
    key_ids = lax.broadcasted_iota(jnp.int32, (1, 1, WIN + QB), 2)
    distance = query_ids + WIN - key_ids
    near_ok = (distance >= 0) & (distance < WIN) & (block_start + key_ids - WIN >= 0)
    far_ok = chosen_now + WIN <= block_start.reshape(1, 1, blocks, 1)
    near_mask = jnp.broadcast_to(
        near_ok[:, None, None], (blocks, buckets, heads_local, QB, WIN + QB)
    )
    far_mask = jnp.broadcast_to(
        jnp.transpose(far_ok, (2, 0, 1, 3))[:, :, :, None, :],
        (blocks, buckets, heads_local, QB, KSEL),
    )
    return (flat_index, jnp.concatenate([near_mask, far_mask], -1))


def attention_setup(queries, key_rows, value_rows, chosen_now, seq_start, seq_first):
    length_local, buckets, feature_width = queries.shape
    heads_local = feature_width // HDIM
    blocks = length_local // QB
    query_blocks = queries.reshape(blocks, QB, buckets, heads_local, HDIM)
    flat_index, key_mask = key_geometry(chosen_now, seq_start, blocks)
    near_keys = near_slabs(key_rows, seq_start, seq_first, length_local)
    near_values = near_slabs(value_rows, seq_start, seq_first, length_local)
    far_keys = far_rows(key_rows, flat_index)
    far_values = far_rows(value_rows, flat_index)
    near_scores = jnp.einsum(
        "bqnhe,btnhe->bnhqt", query_blocks, near_keys, preferred_element_type=jnp.float32
    )
    far_scores = jnp.einsum(
        "bqnhe,nhbke->bnhqk", query_blocks, far_keys, preferred_element_type=jnp.float32
    )
    scores = jnp.where(
        key_mask, HDIM ** (-0.5) * jnp.concatenate([near_scores, far_scores], -1), MASKED
    )
    return (query_blocks, near_keys, near_values, far_keys, far_values, flat_index, scores)


def attend(queries, key_rows, value_rows, chosen_now, seq_start, seq_first):
    query_blocks, near_keys, near_values, far_keys, far_values, flat_index, scores = (
        attention_setup(queries, key_rows, value_rows, chosen_now, seq_start, seq_first)
    )
    span = WIN + QB
    row_top = jnp.max(scores, -1, keepdims=True)
    exp_terms = jnp.exp(scores - row_top)
    row_total = jnp.sum(exp_terms, -1, keepdims=True)
    softmax_low = (exp_terms / row_total).astype(jnp.bfloat16)
    near_part = jnp.einsum(
        "bnhqt,btnhe->bqnhe",
        softmax_low[..., :span],
        near_values,
        preferred_element_type=jnp.float32,
    )
    far_part = jnp.einsum(
        "bnhqk,nhbke->bqnhe",
        softmax_low[..., span:],
        far_values,
        preferred_element_type=jnp.float32,
    )
    return ((near_part + far_part).reshape(queries.shape), row_top + jnp.log(row_total))


def spread_back(near_grad, far_grad, flat_index, seq_start, seq_first, total_rows):
    blocks, span, buckets, heads_local, head_size = near_grad.shape
    length_local = blocks * QB
    feature_width = heads_local * head_size
    segment = jnp.zeros((length_local + WIN, buckets, heads_local, head_size), jnp.float32)
    for offset_index in range(WIN // QB + 1):
        piece = near_grad[:, offset_index * QB : (offset_index + 1) * QB].reshape(
            length_local, buckets, heads_local, head_size
        )
        segment = segment.at[offset_index * QB : offset_index * QB + length_local].add(piece)
    full_rows = jnp.zeros((total_rows * buckets * heads_local, head_size), jnp.float32)
    full_rows = full_rows.at[flat_index.reshape(-1)].add(far_grad.reshape(-1, head_size))
    full_rows = full_rows.reshape(total_rows, buckets, feature_width)
    local_part = segment[WIN:].reshape(length_local, buckets, feature_width)
    earlier = jnp.where(seq_first, 0.0, segment[:WIN].reshape(WIN, buckets, feature_width))
    full_rows = lax.dynamic_update_slice_in_dim(
        full_rows,
        lax.dynamic_slice_in_dim(full_rows, seq_start, length_local, 0) + local_part,
        seq_start,
        0,
    )
    earlier_start = jnp.maximum(seq_start - WIN, 0)
    full_rows = lax.dynamic_update_slice_in_dim(
        full_rows,
        lax.dynamic_slice_in_dim(full_rows, earlier_start, WIN, 0) + earlier,
        earlier_start,
        0,
    )
    return full_rows


def attend_back(
    queries, key_rows, value_rows, chosen_now, seq_start, seq_first, log_total, grad_mixed
):
    query_blocks, near_keys, near_values, far_keys, far_values, flat_index, scores = (
        attention_setup(queries, key_rows, value_rows, chosen_now, seq_start, seq_first)
    )
    span = WIN + QB
    score_scale = HDIM ** (-0.5)
    grad_blocks = grad_mixed.reshape(query_blocks.shape)
    weights_full = jnp.exp(scores - log_total)
    softmax_low = weights_full.astype(jnp.bfloat16)
    grad_near_weights = jnp.einsum(
        "bqnhe,btnhe->bnhqt", grad_blocks, near_values, preferred_element_type=jnp.float32
    )
    grad_far_weights = jnp.einsum(
        "bqnhe,nhbke->bnhqk", grad_blocks, far_values, preferred_element_type=jnp.float32
    )
    grad_weights = jnp.concatenate([grad_near_weights, grad_far_weights], -1)
    row_dot = jnp.sum(weights_full * grad_weights, -1, keepdims=True)
    grad_scores = (weights_full * (grad_weights - row_dot)).astype(jnp.bfloat16)
    grad_near, grad_far = (grad_scores[..., :span], grad_scores[..., span:])
    grad_queries = score_scale * (
        jnp.einsum("bnhqt,btnhe->bqnhe", grad_near, near_keys, preferred_element_type=jnp.float32)
        + jnp.einsum("bnhqk,nhbke->bqnhe", grad_far, far_keys, preferred_element_type=jnp.float32)
    )
    near_key_grad = score_scale * jnp.einsum(
        "bnhqt,bqnhe->btnhe", grad_near, query_blocks, preferred_element_type=jnp.float32
    )
    far_key_grad = score_scale * jnp.einsum(
        "bnhqk,bqnhe->nhbke", grad_far, query_blocks, preferred_element_type=jnp.float32
    )
    near_value_grad = jnp.einsum(
        "bnhqt,bqnhe->btnhe",
        softmax_low[..., :span],
        grad_blocks,
        preferred_element_type=jnp.float32,
    )
    far_value_grad = jnp.einsum(
        "bnhqk,bqnhe->nhbke",
        softmax_low[..., span:],
        grad_blocks,
        preferred_element_type=jnp.float32,
    )
    total_rows = key_rows.shape[0]
    key_grad = spread_back(
        near_key_grad, far_key_grad, flat_index, seq_start, seq_first, total_rows
    )
    value_grad = spread_back(
        near_value_grad, far_value_grad, flat_index, seq_start, seq_first, total_rows
    )
    return (grad_queries.reshape(queries.shape), key_grad, value_grad)


def forward_pass(hidden, params, chosen_now, query_mask, seq_start, seq_first, finish):
    (
        ln1_gain,
        ln1_shift,
        w_qkv,
        b_qv,
        w_out,
        b_out,
        ln2_gain,
        ln2_shift,
        w_fc,
        b_fc,
        w_proj,
        b_proj,
    ) = params
    hidden_wide = hidden.astype(jnp.float32)
    normed_all = gather_rows(layer_norm(hidden_wide, ln1_gain, ln1_shift).astype(jnp.bfloat16))
    projected = jnp.einsum("pnd,jdc->jpnc", normed_all, w_qkv, preferred_element_type=jnp.float32)
    queries = (projected[0] + b_qv[0]).astype(jnp.bfloat16)
    key_rows, value_rows = (
        lax.all_gather(projected[1].astype(jnp.bfloat16), "seq", axis=0, tiled=True),
        lax.all_gather((projected[2] + b_qv[1]).astype(jnp.bfloat16), "seq", axis=0, tiled=True),
    )
    attended, log_total = attend(queries, key_rows, value_rows, chosen_now, seq_start, seq_first)
    mixed_rows = (attended * query_mask[:, :, None]).astype(jnp.bfloat16)
    middle = hidden_wide + scatter_product(mixed_rows, w_out, "pnc,cd->pnd") + b_out
    normed_mlp = gather_rows(layer_norm(middle, ln2_gain, ln2_shift).astype(jnp.bfloat16))
    pre_active = (
        jnp.einsum("pnd,df->pnf", normed_mlp, w_fc, preferred_element_type=jnp.float32) + b_fc
    )
    active = gelu_tanh(pre_active).astype(jnp.bfloat16)
    if not finish:
        return (
            normed_all,
            queries,
            key_rows,
            value_rows,
            log_total,
            mixed_rows,
            middle,
            normed_mlp,
            pre_active,
            active,
        )
    output = (middle + scatter_product(active, w_proj, "pnf,fd->pnd") + b_proj).astype(jnp.bfloat16)
    return (output, (key_rows, value_rows))


def backward_pass(hidden, upstream, params, chosen_now, query_mask, seq_start, seq_first):
    (
        ln1_gain,
        ln1_shift,
        w_qkv,
        b_qv,
        w_out,
        b_out,
        ln2_gain,
        ln2_shift,
        w_fc,
        b_fc,
        w_proj,
        b_proj,
    ) = params
    (
        normed_all,
        queries,
        key_rows,
        value_rows,
        log_total,
        mixed_rows,
        middle,
        normed_mlp,
        pre_active,
        active,
    ) = forward_pass(hidden, params, chosen_now, query_mask, seq_start, seq_first, False)
    upstream_all = gather_rows(upstream)
    grad_w_proj = jnp.einsum(
        "pnf,pnd->fd", active, upstream_all, preferred_element_type=jnp.float32
    )
    grad_b_proj = jnp.sum(upstream.astype(jnp.float32), axis=(0, 1))
    grad_active = jnp.einsum(
        "pnd,fd->pnf", upstream_all, w_proj, preferred_element_type=jnp.float32
    )
    unused_value, gelu_pull = jax.vjp(gelu_tanh, pre_active)
    grad_pre = gelu_pull(grad_active)[0].astype(jnp.bfloat16)
    grad_w_fc = jnp.einsum("pnd,pnf->df", normed_mlp, grad_pre, preferred_element_type=jnp.float32)
    grad_b_fc = jnp.sum(grad_pre.astype(jnp.float32), axis=(0, 1))
    grad_normed_mlp = scatter_product(grad_pre, w_fc, "pnf,df->pnd")
    unused_norm, second_pull = jax.vjp(layer_norm, middle, ln2_gain, ln2_shift)
    grad_mid_norm, grad_ln2_gain, grad_ln2_shift = second_pull(grad_normed_mlp)
    grad_middle = upstream.astype(jnp.float32) + grad_mid_norm
    grad_branch = grad_middle.astype(jnp.bfloat16)
    grad_b_out = jnp.sum(grad_branch.astype(jnp.float32), axis=(0, 1))
    branch_all = gather_rows(grad_branch)
    grad_w_out = jnp.einsum(
        "pnc,pnd->cd", mixed_rows, branch_all, preferred_element_type=jnp.float32
    )
    grad_mixed = jnp.einsum(
        "pnd,cd->pnc", branch_all, w_out, preferred_element_type=jnp.float32
    ).astype(jnp.bfloat16) * query_mask[:, :, None].astype(jnp.bfloat16)
    grad_queries, key_grad_all, value_grad_all = attend_back(
        queries, key_rows, value_rows, chosen_now, seq_start, seq_first, log_total, grad_mixed
    )
    key_grad, value_grad = (
        lax.psum_scatter(
            key_grad_all.astype(jnp.bfloat16), "seq", scatter_dimension=0, tiled=True
        ).astype(jnp.float32),
        lax.psum_scatter(
            value_grad_all.astype(jnp.bfloat16), "seq", scatter_dimension=0, tiled=True
        ).astype(jnp.float32),
    )
    grad_project = jnp.stack(
        [
            grad_queries.astype(jnp.bfloat16),
            key_grad.astype(jnp.bfloat16),
            value_grad.astype(jnp.bfloat16),
        ],
        2,
    )
    grad_w_qkv = jnp.einsum(
        "pnd,pnjc->jdc", normed_all, grad_project, preferred_element_type=jnp.float32
    )
    grad_b_qv = jnp.sum(grad_project[:, :, 0::2].astype(jnp.float32), axis=(0, 1))
    grad_normed = scatter_product(grad_project, w_qkv, "pnjc,jdc->pnd")
    unused_first, first_pull = jax.vjp(layer_norm, hidden.astype(jnp.float32), ln1_gain, ln1_shift)
    grad_in_norm, grad_ln1_gain, grad_ln1_shift = first_pull(grad_normed)
    grad_hidden = (grad_middle + grad_in_norm).astype(jnp.bfloat16)
    block_grads = (
        grad_ln1_gain,
        grad_ln1_shift,
        grad_w_qkv,
        grad_b_qv,
        grad_w_out,
        grad_b_out,
        grad_ln2_gain,
        grad_ln2_shift,
        grad_w_fc,
        grad_b_fc,
        grad_w_proj,
        grad_b_proj,
    )
    return (grad_hidden, block_grads)


def on_device(
    inputs,
    cotangent,
    lengths,
    chosen,
    ln1_gain,
    ln1_shift,
    w_qkv,
    b_qv,
    w_out,
    b_out,
    ln2_gain,
    ln2_shift,
    w_fc,
    b_fc,
    w_proj,
    b_proj,
):
    params = tuple(
        (
            weight_array[0]
            for weight_array in (
                ln1_gain,
                ln1_shift,
                w_qkv,
                b_qv,
                w_out,
                b_out,
                ln2_gain,
                ln2_shift,
                w_fc,
                b_fc,
                w_proj,
                b_proj,
            )
        )
    )
    section_index = lax.axis_index("section")
    section_count = lax.axis_size("section")
    seq_index = lax.axis_index("seq")
    tensor_index = lax.axis_index("tensor")
    tensor_count = lax.axis_size("tensor")
    micro_count, rows_local, buckets, feature_width = inputs.shape
    length_local = rows_local * tensor_count
    heads_width = w_qkv.shape[-1]
    seq_start = seq_index * length_local
    seq_first = seq_index == 0
    positions = seq_start + lax.broadcasted_iota(jnp.int32, (micro_count, length_local, buckets), 1)
    mask_all = (positions < lengths[:, None, :]).astype(jnp.float32)
    mask_rows = lax.dynamic_slice_in_dim(mask_all, tensor_index * rows_local, rows_local, 1)
    step_count = micro_count + section_count - 1
    chosen_section = chosen[0]
    received = jnp.zeros((rows_local, buckets, feature_width), jnp.bfloat16)
    stored = jnp.zeros((micro_count, rows_local, buckets, feature_width), jnp.bfloat16)
    outputs = jnp.zeros_like(stored)
    for step_index in range(step_count):
        micro_index = step_index - section_index
        running = (micro_index >= 0) & (micro_index < micro_count)
        slot_index = jnp.clip(micro_index, 0, micro_count - 1)
        block_in = jnp.where(
            section_index == 0, lax.dynamic_index_in_dim(inputs, slot_index, 0, False), received
        )
        chosen_now = lax.dynamic_index_in_dim(chosen_section, slot_index, 0, False)
        query_mask = lax.dynamic_index_in_dim(mask_all, slot_index, 0, False)
        result, key_pair = forward_pass(
            block_in, params, chosen_now, query_mask, seq_start, seq_first, True
        )
        stored = jnp.where(
            running, lax.dynamic_update_index_in_dim(stored, block_in, slot_index, 0), stored
        )
        outputs = jnp.where(
            running, lax.dynamic_update_index_in_dim(outputs, result, slot_index, 0), outputs
        )
        received = from_behind(result, "section", 1)
    back_received = jnp.zeros((rows_local, buckets, feature_width), jnp.bfloat16)
    in_grads = jnp.zeros_like(stored)
    totals = None
    for step_index in range(step_count):
        micro_index = step_index - (section_count - 1 - section_index)
        running = (micro_index >= 0) & (micro_index < micro_count)
        slot_index = jnp.clip(micro_index, 0, micro_count - 1)
        chosen_now = lax.dynamic_index_in_dim(chosen_section, slot_index, 0, False)
        query_mask = lax.dynamic_index_in_dim(mask_all, slot_index, 0, False)
        local_mask = lax.dynamic_index_in_dim(mask_rows, slot_index, 0, False)
        top_grad = (
            lax.dynamic_index_in_dim(cotangent, slot_index, 0, False).astype(jnp.float32)
            * local_mask[:, :, None]
        ).astype(jnp.bfloat16)
        upstream = jnp.where(section_index == section_count - 1, top_grad, back_received)
        hidden = lax.dynamic_index_in_dim(stored, slot_index, 0, False)
        grad_hidden, block_grads = backward_pass(
            hidden, upstream, params, chosen_now, query_mask, seq_start, seq_first
        )
        block_grads = tuple(
            (jnp.where(running, grad_part, jnp.zeros_like(grad_part)) for grad_part in block_grads)
        )
        totals = (
            block_grads
            if step_index == 0
            else tuple(
                (total_part + grad_part for total_part, grad_part in zip(totals, block_grads))
            )
        )
        in_grads = jnp.where(
            running, lax.dynamic_update_index_in_dim(in_grads, grad_hidden, slot_index, 0), in_grads
        )
        back_received = from_behind(grad_hidden, "section", -1)
    (
        sum_ln1_gain,
        sum_ln1_shift,
        sum_w_qkv,
        sum_b_qv,
        sum_w_out,
        sum_b_out,
        sum_ln2_gain,
        sum_ln2_shift,
        sum_w_fc,
        sum_b_fc,
        sum_w_proj,
        sum_b_proj,
    ) = totals
    part_qkv, part_out, part_fc, part_proj = (
        lax.psum_scatter(
            sum_w_qkv.astype(jnp.bfloat16), "seq", scatter_dimension=1, tiled=True
        ).astype(jnp.float32),
        lax.psum_scatter(
            sum_w_out.astype(jnp.bfloat16), "seq", scatter_dimension=1, tiled=True
        ).astype(jnp.float32),
        lax.psum_scatter(
            sum_w_fc.astype(jnp.bfloat16), "seq", scatter_dimension=0, tiled=True
        ).astype(jnp.float32),
        lax.psum_scatter(
            sum_w_proj.astype(jnp.bfloat16), "seq", scatter_dimension=1, tiled=True
        ).astype(jnp.float32),
    )
    bias_qv = lax.dynamic_update_slice_in_dim(
        jnp.zeros((2, feature_width), jnp.float32), sum_b_qv, tensor_index * heads_width, 1
    )
    units_local = sum_b_fc.shape[0]
    bias_fc = lax.dynamic_update_slice_in_dim(
        jnp.zeros((units_local * tensor_count,), jnp.float32),
        sum_b_fc,
        tensor_index * units_local,
        0,
    )
    small_sums = lax.psum(
        (
            sum_ln1_gain,
            sum_ln1_shift,
            bias_qv,
            sum_b_out,
            sum_ln2_gain,
            sum_ln2_shift,
            bias_fc,
            sum_b_proj,
        ),
        ("seq", "tensor"),
    )
    return (
        outputs[None],
        in_grads[None],
        small_sums[0][None],
        small_sums[1][None],
        part_qkv[None],
        small_sums[2][None],
        part_out[None],
        small_sums[3][None],
        small_sums[4][None],
        small_sums[5][None],
        part_fc[None],
        small_sums[6][None],
        part_proj[None],
        small_sums[7][None],
    )


STREAMS = 2
NRM, NMLP, UPS, BRN, ACT, GPRE, HEADS = range(7)
F32 = jnp.float32
LOW = jnp.bfloat16
MESH_ID = pl.DeviceIdType.MESH


def dot_nn(left, right):
    return lax.dot_general(left, right, (((1,), (0,)), ((), ())), preferred_element_type=F32)


def dot_nt(left, right):
    return lax.dot_general(left, right, (((1,), (1,)), ((), ())), preferred_element_type=F32)


def dot_tn(left, right):
    return lax.dot_general(left, right, (((0,), (0,)), ((), ())), preferred_element_type=F32)


def standard(rows):
    centred = rows - jnp.mean(rows, axis=-1, keepdims=True)
    scale = lax.rsqrt(jnp.mean(centred * centred, axis=-1, keepdims=True) + NORM_EPS)
    return centred * scale, scale


def standard_back(grad, xhat, scale):
    inner = jnp.mean(grad * xhat, axis=-1, keepdims=True)
    return scale * (grad - jnp.mean(grad, axis=-1, keepdims=True) - xhat * inner)


def column_sum(rows):
    return jnp.sum(rows.astype(F32), axis=0, keepdims=True)


def relay_kernel(names, *refs):
    r = types.SimpleNamespace(**dict(zip(names, refs)))
    a, c, t = (lax.axis_index(name) for name in ("section", "seq", "tensor"))
    lines = lax.axis_size("section")
    chips = lax.axis_size("tensor")
    rows, buckets, width = r.inputs.shape[1:]
    half_width = width // 2
    local = rows * chips
    total = 2 * local
    sub = rows // STREAMS
    stream_rows = local // STREAMS
    head_width = r.wo_in.shape[0]
    heads = head_width // HDIM
    blocks = local // QB
    units = r.wp_in.shape[0]
    scale = HDIM ** (-0.5)
    streams = range(STREAMS)
    kv_lanes = slice(2 * head_width, 4 * head_width)
    value_bias = slice(3 * head_width, 4 * head_width)

    def remote(src, dst, send, recv, **target):
        return pltpu.make_async_remote_copy(
            src_ref=src,
            dst_ref=dst,
            send_sem=send,
            recv_sem=recv,
            device_id=target,
            device_id_type=MESH_ID,
        )

    def drain(ref, sem):
        pltpu.make_async_copy(ref, ref, sem).wait()

    def row_block(index, size):
        return pl.ds(pl.multiple_of(index * size, size), size)

    mine = row_block(t, sub)
    my_half = row_block(c, local)

    barrier = pltpu.get_barrier_semaphore()
    for core in range(2):
        for step in range(1, chips):
            there = {"tensor": (t + step) % chips, "seq": core}
            pl.semaphore_signal(barrier, inc=1, device_id=there, device_id_type=MESH_ID)
        for step in range(1, lines):
            there = {"section": (a + step) % lines, "seq": core}
            pl.semaphore_signal(barrier, inc=1, device_id=there, device_id_type=MESH_ID)
    pl.semaphore_signal(barrier, inc=1, device_id={"seq": 1 - c}, device_id_type=MESH_ID)
    pl.semaphore_wait(barrier, 2 * (chips - 1) + 2 * (lines - 1) + 1)

    def beside(s):
        return s + 1 - 2 * (s % 2)

    def above(s):
        return (s + 2) % 4

    def store(p):
        return (r.wq, r.wo, r.wf, r.wp)[p]

    def source(p):
        return (r.wq_in, r.wo_in, r.wf_in, r.wp_in)[p]

    def height(p):
        return source(p).shape[0]

    def core_half(p, s, core):
        return store(p).at[s, row_block(core, height(p) // 2)]

    def first_hop(p, s, neighbour, which):
        return remote(
            source(p).at[row_block(c, height(p) // 2)],
            core_half(p, s, c),
            r.w_first_s.at[p, which],
            r.w_first_r.at[s, p],
            section=neighbour,
        )

    def second_hop(p, s, which):
        view = store(p).at[s, row_block(2 * c + which, height(p) // 4)]
        return remote(
            view, view, r.w_second_s.at[s, p], r.w_second_r.at[s, p, which], section=3 - s
        )

    def core_hop(p, s, core):
        view = core_half(p, s, core)
        return remote(view, view, r.w_core_s.at[s, p], r.w_core_r.at[s, p], seq=1 - c)

    def own_copy(p):
        return pltpu.make_async_copy(source(p), store(p).at[a], r.w_own.at[p])

    def pass_on(s, p):
        for which, line in enumerate((beside(s), above(s))):

            @pl.when(a == line)
            def _():
                first_hop(p, s, line, which).wait_recv()
                second_hop(p, s, which).start()
                core_hop(p, s, c).start()

    def pass_far(s, p):
        @pl.when(a == 3 - s)
        def _():
            second_hop(p, s, 0).wait_recv()
            second_hop(p, s, 1).wait_recv()
            core_hop(p, s, c).start()

    def need(s, p):
        @pl.when(s == 0)
        def _():
            pass_on(s, p)
            pass_far(s, p)

        @pl.when(a == s)
        def _():
            own_copy(p).wait()

        @pl.when(a != s)
        def _():
            core_hop(p, s, 1 - c).wait_recv()

    def small_copy(step, line, slot):
        return remote(
            r.small_own, r.small.at[slot], r.small_s.at[step], r.small_r.at[slot], section=line
        )

    def count_copy(step, line, slot):
        return remote(
            r.count_own.at[line],
            r.count.at[slot],
            r.count_s.at[step],
            r.count_r.at[slot],
            section=line,
        )

    singles = (r.ln1_gain, r.ln1_shift, r.ln2_gain, r.ln2_shift, r.b_out, r.b_proj)
    for place, single in enumerate(singles):
        r.small_own[place : place + 1] = single[...]
    r.small_own[6:7, :units] = r.b_fc[...]
    r.small_own[7:8] = jnp.zeros((1, width), F32)
    r.small_own[7:8, 0:head_width] = r.b_qv[0:1]
    r.small_own[7:8, value_bias] = r.b_qv[1:2]
    for step in range(1, lines):
        small_copy(step - 1, (a + step) % lines, a).start()
    for p in range(4):
        for which, line in enumerate((beside(a), above(a))):
            first_hop(p, a, line, which).start()
    for p in range(4):
        own_copy(p).start()
    r.small[a] = r.small_own[...]

    def place_of(index):
        inside = index % local
        stream, left = inside // stream_rows, inside % stream_rows
        return (index // local) * local + (left // sub) * rows + stream * sub + left % sub

    def iota(shape, dimension):
        return lax.broadcasted_iota(jnp.int32, shape, dimension)

    square = jnp.where(iota((KSEL, KSEL), 0) == iota((KSEL, KSEL), 1), 1.0, 0.0).astype(LOW)
    position = place_of(iota((KSEL, total), 1)).astype(F32)
    for pair in range(lines * heads):
        line, head = pair // heads, pair % heads
        columns = dot_nt(square, r.chosen[pair].astype(F32).astype(LOW))
        for block in range(blocks):
            pick = head * blocks + block
            r.count_own[line, pick : pick + 1, :] = jnp.sum(
                jnp.where(columns[:, block : block + 1] == position, 1.0, 0.0),
                axis=0,
                keepdims=True,
            )
    for step in range(1, lines):
        count_copy(step - 1, (a + step) % lines, a).start()
    r.count[a] = r.count_own[a]

    partners = (3 - t, (t + 2) % 4, t + 1 - 2 * (t % 2))

    def gather(buffer, s, kind, j, slot, chip):
        view = buffer.at[s, j, row_block(chip, sub)]
        return remote(
            view,
            view,
            r.ag_s.at[kind, j, slot],
            r.ag_r.at[kind, j, slot],
            tensor=partners[slot],
        )

    def gather_start(buffer, s, kind, j):
        for slot in range(chips - 1):
            gather(buffer, s, kind, j, slot, t).start()

    def gather_wait(buffer, s, kind, j):
        for slot in range(chips - 1):
            gather(buffer, s, kind, j, slot, partners[slot]).wait_recv()
        for slot in range(chips - 1):
            gather(buffer, s, kind, j, slot, t).wait_send()

    def scatter(s, kind, j, slot):
        return remote(
            r.part.at[kind, j, row_block(partners[slot], sub)],
            r.arrived.at[s, kind, j, slot],
            r.rs_s.at[kind, j, slot],
            r.rs_r.at[kind, j, slot],
            tensor=partners[slot],
        )

    def scatter_start(s, kind, j, product):
        r.part[kind, j] = product.astype(LOW)
        for slot in range(chips - 1):
            scatter(s, kind, j, slot).start()

    def scatter_sum(s, kind, j):
        result = r.part[kind, j, mine].astype(F32)
        for slot in range(chips - 1):
            scatter(s, kind, j, slot).wait_recv()
            result = result + r.arrived[s, kind, j, slot].astype(F32)
        for slot in range(chips - 1):
            scatter(s, kind, j, slot).wait_send()
        return result

    own_rows = (r.nrm, r.nmlp, r.ups, r.brn, r.act, r.gpre, r.hds)
    all_rows = (
        r.all_nrm,
        r.all_nmlp,
        r.all_ups,
        r.all_brn,
        r.all_act,
        r.all_gpre,
        r.all_hds,
    )

    def rows_copy(index, s, same, stays=False):
        core = c if same else 1 - c
        src = own_rows[index].at[s]
        dst = all_rows[index].at[a, c]
        if index <= BRN:
            src = src.at[:, :, row_block(core, half_width)]
        recv = r.rows_r.at[index]
        if stays:
            return pltpu.make_async_copy(src, dst, recv)
        if same:
            return remote(src, dst, r.rows_s.at[index, s, 0], recv, section=s)
        return remote(src, dst, r.rows_s.at[index, s, 1], recv, section=s, seq=1 - c)

    def rows_start(index, s):
        @pl.when(a == s)
        def _():
            rows_copy(index, s, True, True).start()

        @pl.when(a != s)
        def _():
            rows_copy(index, s, True).start()

        if index <= BRN:
            rows_copy(index, s, False).start()

    def rows_sent(index, s):
        @pl.when(a != s)
        def _():
            rows_copy(index, s, True).wait_send()

        if index <= BRN:
            rows_copy(index, s, False).wait_send()

    def share_copy(index, core):
        view = all_rows[index].at[:, core]
        return remote(view, view, r.share_s.at[index - ACT], r.share_r.at[index - ACT], seq=1 - c)

    def share(index):
        drain(all_rows[index].at[:, c], r.rows_r.at[index])
        share_copy(index, c).start()

    def home_copy(src, dst, send, recv, s):
        return remote(src.at[s], dst.at[a], send.at[s], recv, section=s)

    def home_start(src, dst, send, recv, s):
        @pl.when(a == s)
        def _():
            pltpu.make_async_copy(src.at[s], dst.at[a], recv).start()

        @pl.when(a != s)
        def _():
            home_copy(src, dst, send, recv, s).start()

    def home_sent(*what):
        @pl.when(a != what[-1])
        def _():
            home_copy(*what).wait_send()

    out_home = (r.out_low, r.acts, r.out_s, r.out_r)
    grad_home = (r.grad_low, r.grads, r.grad_s, r.grad_r)
    norm_home = (r.norm_part, r.norm_all, r.norm_s, r.norm_r)

    length = r.lengths[a // buckets, a % buckets]
    query = place_of(c * local + iota((local, total), 0))
    key = place_of(iota((local, total), 1))
    near = jnp.where((query >= key) & (query - key < WIN), 1.0, 0.0)
    key_row = place_of(iota((1, total), 1))
    block_of = place_of(iota((local, total), 0)) // QB
    first_block = jnp.where(block_of == 0, 1.0, 0.0)

    def row_mask(place):
        return jnp.where(place < length, 1.0, 0.0)

    def multiplicity(s, head):
        times = near
        for block in range(blocks):
            pick = head * blocks + block
            limit = (c * blocks + block) * QB - WIN
            counted = jnp.where(key_row <= limit, r.count[s, pick : pick + 1, :], 0.0)
            times = times + jnp.where(block_of == block, counted, 0.0)
        return times

    def head_cols(head):
        return slice(head * HDIM, (head + 1) * HDIM)

    def kv_copy(s, core):
        view = r.kv.at[s, row_block(core, local)]
        return remote(view, view, r.kv_s.at[s], r.kv_r.at[s], seq=1 - c)

    def dkv_copy(s):
        return remote(r.dkv_out.at[s], r.dkv_in.at[s], r.dkv_s.at[s], r.dkv_r.at[s], seq=1 - c)

    def flat(array):
        return array.reshape(local, array.shape[-1])

    def own_sequence(ref):
        both = ref[a // buckets].astype(F32)
        picked = both[:, 0, :]
        for bucket in range(1, buckets):
            picked = jnp.where(a % buckets == bucket, both[:, bucket, :], picked)
        return picked

    def part_rows(j):
        return slice(j * sub, (j + 1) * sub)

    r.hidden[...] = own_sequence(r.inputs)
    own_place = c * local + t * rows + iota((rows, 1), 0)
    r.upstream[...] = (own_sequence(r.cotangent) * row_mask(own_place)).astype(LOW)
    r.norm_part[...] = jnp.zeros_like(r.norm_part)

    def enter(s, j):
        xhat, inverse = standard(r.hidden[part_rows(j)])
        r.xhat1[s, j] = xhat
        r.inv1[s, j] = jnp.broadcast_to(inverse, (sub, 128))
        r.nrm[s, j, mine] = (xhat * r.small[s, 0:1] + r.small[s, 1:2]).astype(LOW)
        gather_start(r.nrm, s, 0, j)

    def project(s, j):
        gather_wait(r.nrm, s, 0, j)
        normed = r.nrm[s, j]
        place = row_block(c * STREAMS + j, stream_rows)
        both = dot_nt(normed, r.wq[s, head_width : 3 * head_width])
        r.kv[s, place] = (both + r.small[s, 7:8, kv_lanes]).astype(LOW)

    def ask(s, j):
        queries = dot_nt(r.nrm[s, j], r.wq[s, 0:head_width]) + r.small[s, 7:8, 0:head_width]
        r.qry[s, j] = queries.astype(LOW)

    def attend_line(s):
        mixed = []
        queries = flat(r.qry[s])
        for head in range(heads):
            times = multiplicity(s, head)
            scores = scale * dot_nt(queries[:, head_cols(head)], r.kv[s, :, head_cols(head)])
            scores = jnp.where(times > 0.0, scores, MASKED)
            top = jnp.max(scores, axis=-1, keepdims=True)
            terms = times * jnp.exp(scores - top)
            weights = terms / jnp.sum(terms, axis=-1, keepdims=True)
            r.soft[s, head] = weights
            mixed.append(dot_nn(weights.astype(LOW), r.kv[s, :, head_cols(heads + head)]))
        mask = row_mask(place_of(c * local + iota((local, 1), 0)))
        mixed = (jnp.concatenate(mixed, axis=-1) * mask).astype(LOW)
        r.mix[...] = mixed.reshape(r.mix.shape)
        r.hds[s, :, :, 3 * head_width :] = mixed.reshape(r.mix.shape)

    def leave_attention(s, j):
        scatter_start(s, 0, j, dot_nn(r.mix[j], r.wo[s]))

    def between(s, j):
        middle = r.hidden[part_rows(j)] + scatter_sum(s, 0, j) + r.small[s, 4:5]
        r.middle[part_rows(j)] = middle
        xhat, inverse = standard(middle)
        r.xhat2[s, j] = xhat
        r.inv2[s, j] = jnp.broadcast_to(inverse, (sub, 128))
        r.nmlp[s, j, mine] = (xhat * r.small[s, 2:3] + r.small[s, 3:4]).astype(LOW)
        gather_start(r.nmlp, s, 1, j)

    def feed(s, j):
        gather_wait(r.nmlp, s, 1, j)
        before = dot_nn(r.nmlp[s, j], r.wf[s]) + r.small[s, 6:7, :units]
        bend = jnp.tanh(0.7978845608028654 * (before + 0.044715 * before * before * before))
        r.act[s, j] = (0.5 * before * (1.0 + bend)).astype(LOW)
        r.slope[s, j] = 0.5 * (1.0 + bend) + 0.5 * before * (1.0 - bend * bend) * (
            0.7978845608028654 * (1.0 + 3 * 0.044715 * before * before)
        )

    def leave_feed(s, j):
        scatter_start(s, 1, j, dot_nn(r.act[s, j], r.wp[s]))

    def finish(s, j):
        result = r.middle[part_rows(j)] + scatter_sum(s, 1, j) + r.small[s, 5:6]
        r.out_low[s, part_rows(j)] = result.astype(LOW)
        r.hidden[part_rows(j)] = result.astype(LOW).astype(F32)

    def small_ready(s):
        @pl.when(a != s)
        def _():
            small_copy(0, a, s).wait_recv()

    small_ready(0)
    for j in streams:
        enter(0, j)

    def forward(s, _):
        need(s, 0)
        for j in streams:
            project(s, j)
        kv_copy(s, c).start()
        for j in streams:
            ask(s, j)
        rows_start(NRM, s)

        @pl.when(a != s)
        def _():
            count_copy(0, a, s).wait_recv()

        kv_copy(s, 1 - c).wait_recv()
        attend_line(s)
        need(s, 1)
        for j in streams:
            leave_attention(s, j)
        for j in streams:
            between(s, j)
        need(s, 2)
        for j in streams:
            feed(s, j)
            if j == 0:
                need(s, 3)
            leave_feed(s, j)
        rows_start(NMLP, s)
        rows_start(ACT, s)

        @pl.when(s + 1 < lines)
        def _():
            small_ready(s + 1)

        for j in streams:
            finish(s, j)

            @pl.when(s + 1 < lines)
            def _():
                enter(s + 1, j)

        home_start(*out_home, s)

        @pl.when(s == 0)
        def _():
            for later in range(1, lines):
                for p in range(4):
                    pass_on(later, p)

        @pl.when(s + 1 < lines)
        def _():
            for p in range(4):
                pass_far(s + 1, p)

        return 0

    lax.fori_loop(0, lines, forward, 0)

    def turn(s, j):
        upstream = r.upstream[part_rows(j)]
        r.ups[s, j, mine] = upstream
        gather_start(r.ups, s, 2, j)
        r.norm_part[s, 5:6] += column_sum(upstream)

    def feed_back(s, j):
        gather_wait(r.ups, s, 2, j)
        grad_pre = (dot_nt(r.ups[s, j], r.wp[s]) * r.slope[s, j]).astype(LOW)
        r.gpre[s, j] = grad_pre
        scatter_start(s, 2, j, dot_nt(grad_pre, r.wf[s]))
        r.norm_part[s, 6:7, :units] += column_sum(grad_pre)

    def between_back(s, j):
        grad = scatter_sum(s, 2, j)
        xhat = r.xhat2[s, j]
        upstream = r.upstream[part_rows(j)].astype(F32)
        grad_middle = upstream + standard_back(
            grad * r.small[s, 2:3], xhat, r.inv2[s, j, :, 0:1]
        )
        r.middle[part_rows(j)] = grad_middle
        branch = grad_middle.astype(LOW)
        r.brn[s, j, mine] = branch
        gather_start(r.brn, s, 3, j)
        r.norm_part[s, 2:3] += column_sum(grad * xhat)
        r.norm_part[s, 3:4] += column_sum(grad)
        r.norm_part[s, 4:5] += column_sum(branch)

    def mixed_back(s, j):
        gather_wait(r.brn, s, 3, j)
        place = place_of(c * local + j * stream_rows + iota((stream_rows, 1), 0))
        r.gmix[j] = (dot_nt(r.brn[s, j], r.wo[s]) * row_mask(place)).astype(LOW)

    def attend_line_back(s):
        grad_q, grad_k, grad_v = [], [], []
        grad_mixed = flat(r.gmix[...])
        queries = flat(r.qry[s])
        for head in range(heads):
            cols = head_cols(head)
            weights = r.soft[s, head]
            grad_head = grad_mixed[:, cols]
            grad_weights = dot_nt(grad_head, r.kv[s, :, head_cols(heads + head)])
            inner = jnp.sum(weights * grad_weights, axis=-1, keepdims=True)
            grad_scores = (weights * (grad_weights - inner)).astype(LOW)
            grad_k.append(scale * dot_tn(grad_scores, queries[:, cols]))
            grad_v.append(dot_tn(weights.astype(LOW), grad_head))
            grad_q.append(scale * dot_nn(grad_scores, r.kv[s, :, cols]))
        r.dkv_all[...] = jnp.concatenate(grad_k + grad_v, axis=-1)
        r.dkv_out[s] = r.dkv_all[row_block(1 - c, local)].astype(LOW)
        dkv_copy(s).start()
        grad_q = jnp.concatenate(grad_q, axis=-1).astype(LOW)
        r.hds[s, :, :, 0:head_width] = grad_q.reshape(r.mix.shape)
        r.norm_part[s, 7:8, 0:head_width] = column_sum(grad_q)
        dkv_copy(s).wait_recv()
        joined = (r.dkv_all[my_half] + r.dkv_in[s].astype(F32)).astype(LOW)
        r.hds[s, :, :, head_width : 3 * head_width] = joined.reshape(
            STREAMS, stream_rows, 2 * head_width
        )
        r.norm_part[s, 7:8, kv_lanes] = column_sum(joined)

    def leave_back(s, j):
        product = dot_nn(r.hds[s, j, :, 0 : 3 * head_width], r.wq[s])
        scatter_start(s, 3, j, product)

    def finish_back(s, j):
        grad = scatter_sum(s, 3, j)
        xhat = r.xhat1[s, j]
        result = r.middle[part_rows(j)] + standard_back(
            grad * r.small[s, 0:1], xhat, r.inv1[s, j, :, 0:1]
        )
        r.upstream[part_rows(j)] = result.astype(LOW)
        r.grad_low[s, part_rows(j)] = result.astype(LOW)
        r.norm_part[s, 0:1] += column_sum(grad * xhat)
        r.norm_part[s, 1:2] += column_sum(grad)

    for j in streams:
        turn(lines - 1, j)

    def backward(index, _):
        s = lines - 1 - index
        for j in streams:
            feed_back(s, j)
        rows_start(UPS, s)
        rows_start(GPRE, s)

        @pl.when(index == 1)
        def _():
            share(ACT)

        for j in streams:
            between_back(s, j)
        for j in streams:
            mixed_back(s, j)
        rows_start(BRN, s)
        attend_line_back(s)
        for j in streams:
            leave_back(s, j)
        rows_start(HEADS, s)
        for j in streams:
            finish_back(s, j)

            @pl.when(s > 0)
            def _():
                turn(s - 1, j)

        home_start(*norm_home, s)
        home_start(*grad_home, s)
        return 0

    lax.fori_loop(0, lines, backward, 0)

    share(GPRE)
    share(HEADS)

    drain(r.norm_all, r.norm_r)
    slot = c * chips + t
    norm_sum = r.norm_all[0]
    for line in range(1, lines):
        norm_sum = norm_sum + r.norm_all[line]
    r.ends[slot] = norm_sum

    def ends_copy(step):
        core, chip = step // chips, step % chips
        view = r.ends.at[slot]
        return remote(
            view,
            view,
            r.ends_s.at[step - 1],
            r.ends_r,
            seq=(c + core) % 2,
            tensor=(t + chip) % chips,
        )

    for step in range(1, 2 * chips):
        ends_copy(step).start()

    for index in range(ACT):
        drain(all_rows[index], r.rows_r.at[index])
    for index in range(ACT, 7):
        share_copy(index, 1 - c).wait_recv()
        share_copy(index, c).wait_send()
    drain(r.acts, r.out_r)
    drain(r.grads, r.grad_r)
    drain(r.ends.at[0 : 2 * chips - 1], r.ends_r)
    for step in range(1, 2 * chips):
        ends_copy(step).wait_send()
    for step in range(1, lines):
        small_copy(step - 1, (a + step) % lines, a).wait_send()
        count_copy(step - 1, (a + step) % lines, a).wait_send()
    for p in range(4):
        for which, line in enumerate((beside(a), above(a))):
            first_hop(p, a, line, which).wait_send()

    def sent(s, _):
        home_sent(*out_home, s)
        home_sent(*grad_home, s)
        home_sent(*norm_home, s)
        kv_copy(s, c).wait_send()
        dkv_copy(s).wait_send()
        for index in range(7):
            rows_sent(index, s)
        for p in range(4):

            @pl.when((a == beside(s)) | (a == above(s)))
            def _():
                second_hop(p, s, 0).wait_send()

            @pl.when(a != s)
            def _():
                core_hop(p, s, c).wait_send()

        return 0

    lax.fori_loop(0, lines, sent, 0)


def relay_call(inputs, cotangent, lengths, chosen, singles, weights):
    lines = lax.axis_size("section")
    chips = lax.axis_size("tensor")
    rows, buckets, width = inputs.shape[1:]
    local, total, half = rows * chips, 2 * rows * chips, width // 2
    head_width, units = weights["wo_in"].shape[0], weights["wp_in"].shape[0]
    heads = head_width // HDIM
    sub, stream = rows // STREAMS, local // STREAMS
    peers = chips - 1
    vmem, dma = pltpu.VMEM, pltpu.SemaphoreType.DMA
    operands = dict(
        inputs=inputs,
        cotangent=cotangent,
        lengths=lengths,
        chosen=chosen,
        **singles,
        **weights,
    )

    def space(name):
        if name in weights:
            return pl.ANY
        return pltpu.SMEM if operands[name] is lengths else pltpu.VMEM

    sums = dict(
        acts=((lines, rows, width), LOW),
        grads=((lines, rows, width), LOW),
        ends=((2 * chips, 8, width), F32),
    )
    gathered = dict(
        all_nrm=((lines, 2, STREAMS, stream, half), LOW),
        all_nmlp=((lines, 2, STREAMS, stream, half), LOW),
        all_ups=((lines, 2, STREAMS, stream, half), LOW),
        all_brn=((lines, 2, STREAMS, stream, half), LOW),
        all_act=((lines, 2, STREAMS, stream, units), LOW),
        all_gpre=((lines, 2, STREAMS, stream, units), LOW),
        all_hds=((lines, 2, STREAMS, stream, 4 * head_width), LOW),
    )
    outputs = dict(**sums, **gathered)
    scratch = dict(
        wq=vmem((lines,) + weights["wq_in"].shape, LOW),
        wo=vmem((lines,) + weights["wo_in"].shape, LOW),
        wf=vmem((lines,) + weights["wf_in"].shape, LOW),
        wp=vmem((lines,) + weights["wp_in"].shape, LOW),
        small_own=vmem((8, width), F32),
        small=vmem((lines, 8, width), F32),
        count_own=vmem((lines, 8, total), F32),
        count=vmem((lines, 8, total), F32),
        hidden=vmem((rows, width), F32),
        middle=vmem((rows, width), F32),
        upstream=vmem((rows, width), LOW),
        xhat1=vmem((lines, STREAMS, sub, width), F32),
        inv1=vmem((lines, STREAMS, sub, 128), F32),
        xhat2=vmem((lines, STREAMS, sub, width), F32),
        inv2=vmem((lines, STREAMS, sub, 128), F32),
        nrm=vmem((lines, STREAMS, stream, width), LOW),
        nmlp=vmem((lines, STREAMS, stream, width), LOW),
        ups=vmem((lines, STREAMS, stream, width), LOW),
        brn=vmem((lines, STREAMS, stream, width), LOW),
        act=vmem((lines, STREAMS, stream, units), LOW),
        gpre=vmem((lines, STREAMS, stream, units), LOW),
        slope=vmem((lines, STREAMS, stream, units), F32),
        mix=vmem((STREAMS, stream, head_width), LOW),
        qry=vmem((lines, STREAMS, stream, head_width), LOW),
        gmix=vmem((STREAMS, stream, head_width), LOW),
        hds=vmem((lines, STREAMS, stream, 4 * head_width), LOW),
        kv=vmem((lines, total, 2 * head_width), LOW),
        soft=vmem((lines, heads, local, total), F32),
        dkv_all=vmem((total, 2 * head_width), F32),
        dkv_out=vmem((lines, local, 2 * head_width), LOW),
        dkv_in=vmem((lines, local, 2 * head_width), LOW),
        part=vmem((4, STREAMS, stream, width), LOW),
        arrived=vmem((lines, 4, STREAMS, peers, sub, width), LOW),
        out_low=vmem((lines, rows, width), LOW),
        grad_low=vmem((lines, rows, width), LOW),
        norm_part=vmem((lines, 8, width), F32),
        norm_all=vmem((lines, 8, width), F32),
        w_first_s=dma((4, 2)),
        w_first_r=dma((lines, 4)),
        w_second_s=dma((lines, 4)),
        w_second_r=dma((lines, 4, 2)),
        w_core_s=dma((lines, 4)),
        w_core_r=dma((lines, 4)),
        w_own=dma((4,)),
        small_s=dma((lines - 1,)),
        small_r=dma((lines,)),
        count_s=dma((lines - 1,)),
        count_r=dma((lines,)),
        ag_s=dma((4, STREAMS, peers)),
        ag_r=dma((4, STREAMS, peers)),
        rs_s=dma((4, STREAMS, peers)),
        rs_r=dma((4, STREAMS, peers)),
        kv_s=dma((lines,)),
        kv_r=dma((lines,)),
        dkv_s=dma((lines,)),
        dkv_r=dma((lines,)),
        rows_s=dma((7, lines, 2)),
        rows_r=dma((7,)),
        share_s=dma((3,)),
        share_r=dma((3,)),
        out_s=dma((lines,)),
        out_r=dma,
        grad_s=dma((lines,)),
        grad_r=dma,
        norm_s=dma((lines,)),
        norm_r=dma,
        ends_s=dma((2 * chips - 1,)),
        ends_r=dma,
    )
    names = tuple(operands) + tuple(outputs) + tuple(scratch)
    results = pl.pallas_call(
        functools.partial(relay_kernel, names),
        out_shape=[jax.ShapeDtypeStruct(shape, kind) for shape, kind in outputs.values()],
        in_specs=[pl.BlockSpec(memory_space=space(name)) for name in operands],
        out_specs=[
            pl.BlockSpec(memory_space=pl.ANY if name in gathered else pltpu.VMEM)
            for name in outputs
        ],
        scratch_shapes=list(scratch.values()),
        compiler_params=pltpu.CompilerParams(
            collective_id=0, has_side_effects=True, vmem_limit_bytes=60 * 2**20
        ),
        name="relay",
    )(*operands.values())
    return dict(zip(outputs, results))


def weights_kernel(names, *refs):
    r = types.SimpleNamespace(**dict(zip(names, refs)))
    step = pl.program_id(0)
    micro_count, rows, buckets, width = r.activations.shape
    chips, units, head_width = r.ends.shape[0] // 2, r.all_act.shape[-1], r.w_out.shape[0]

    @pl.when(step == 0)
    def _():
        sums = r.ends[0]
        for other in range(1, 2 * chips):
            sums = sums + r.ends[other]
        singles = (r.ln1_gain, r.ln1_shift, r.ln2_gain, r.ln2_shift, r.b_out, r.b_proj)
        for place, single in enumerate(singles):
            single[...] = sums[place : place + 1]
        for chip in range(chips):
            both = r.ends[chip] + r.ends[chips + chip]
            r.b_fc[:, chip * units : (chip + 1) * units] = both[6:7, :units]
            here = slice(chip * head_width, (chip + 1) * head_width)
            r.b_qv[0:1, here] = both[7:8, :head_width]
            r.b_qv[1:2, here] = both[7:8, 3 * head_width : 4 * head_width]
        for target, source in ((r.activations, r.acts), (r.in_grads, r.grads)):
            for micro in range(micro_count):
                rows_of = [
                    source[micro * buckets + bucket].astype(F32)[:, None, :]
                    for bucket in range(buckets)
                ]
                target[micro] = jnp.concatenate(rows_of, axis=1).astype(LOW)
        for target in (r.w_qkv, r.w_out, r.w_fc, r.w_proj):
            target[...] = jnp.zeros_like(target)

    def rows_of_sequence(ref):
        return ref[0].reshape(2 * chips * rows, ref.shape[-1])

    nrm, nmlp, ups, brn, act, gpre, hds = (
        rows_of_sequence(ref)
        for ref in (r.all_nrm, r.all_nmlp, r.all_ups, r.all_brn, r.all_act, r.all_gpre, r.all_hds)
    )
    r.w_proj[...] += dot_tn(act, ups)
    r.w_fc[...] += dot_tn(nmlp, gpre)
    r.w_out[...] += dot_tn(hds[:, 3 * head_width :], brn)
    r.w_qkv[...] += dot_tn(hds[:, 0 : 3 * head_width], nrm)


def weights_call(relayed, inputs_shape, head_width, units):
    lines = lax.axis_size("section")
    chips = lax.axis_size("tensor")
    width = inputs_shape[-1]
    half = width // 2
    outputs = dict(
        activations=(inputs_shape, LOW),
        in_grads=(inputs_shape, LOW),
        ln1_gain=((1, width), F32),
        ln1_shift=((1, width), F32),
        w_qkv=((3 * head_width, half), F32),
        b_qv=((2, width), F32),
        w_out=((head_width, half), F32),
        b_out=((1, width), F32),
        ln2_gain=((1, width), F32),
        ln2_shift=((1, width), F32),
        w_fc=((half, units), F32),
        b_fc=((1, chips * units), F32),
        w_proj=((units, half), F32),
        b_proj=((1, width), F32),
    )

    def spec(array):
        if len(array.shape) < 5:
            return pl.BlockSpec(array.shape, lambda step: (0,) * len(array.shape))
        return pl.BlockSpec(
            (1,) + array.shape[1:], lambda step: (step,) + (0,) * (len(array.shape) - 1)
        )

    def whole(shape):
        return pl.BlockSpec(shape, lambda step: (0,) * len(shape))

    return pl.pallas_call(
        functools.partial(weights_kernel, tuple(relayed) + tuple(outputs)),
        out_shape=[jax.ShapeDtypeStruct(shape, kind) for shape, kind in outputs.values()],
        grid=(lines,),
        in_specs=[spec(array) for array in relayed.values()],
        out_specs=[whole(shape) for shape, _ in outputs.values()],
        compiler_params=pltpu.CompilerParams(vmem_limit_bytes=60 * 2**20),
        name="weight_gradients",
    )(*relayed.values())


def on_line(
    inputs,
    cotangent,
    lengths,
    chosen,
    ln1_gain,
    ln1_shift,
    w_qkv,
    b_qv,
    w_out,
    b_out,
    ln2_gain,
    ln2_shift,
    w_fc,
    b_fc,
    w_proj,
    b_proj,
):
    head_width, units = w_out.shape[1], w_fc.shape[2]
    singles = dict(
        ln1_gain=ln1_gain,
        ln1_shift=ln1_shift,
        ln2_gain=ln2_gain,
        ln2_shift=ln2_shift,
        b_out=b_out,
        b_proj=b_proj,
        b_fc=b_fc,
        b_qv=b_qv[0],
    )
    weights = dict(
        wq_in=jnp.swapaxes(w_qkv[0], 1, 2).reshape(-1, inputs.shape[-1]),
        wo_in=w_out[0],
        wf_in=w_fc[0],
        wp_in=w_proj[0],
    )
    picks = chosen.reshape((-1,) + chosen.shape[-2:])
    relayed = relay_call(inputs, cotangent, lengths, picks, singles, weights)
    results = list(weights_call(relayed, inputs.shape, head_width, units))
    results[4] = jnp.swapaxes(results[4].reshape(3, head_width, -1), 1, 2)
    vectors = (2, 3, 7, 8, 9, 11, 13)
    return tuple(
        result if place in vectors else result[None] for place, result in enumerate(results)
    )


def fits_lines(mesh):
    return mesh.shape["section"] == 4 and mesh.shape["seq"] == 2 and mesh.shape["tensor"] == 4


def solution(mesh):
    placed = (
        P(None, ("seq", "tensor"), None, None),
        P(None, ("seq", "tensor"), None, None),
        P(),
        P("section", None, None, "tensor", "seq", None),
        P("section", None),
        P("section", None),
        P("section", None, None, "tensor"),
        P("section", None, "tensor"),
        P("section", "tensor", None),
        P("section", None),
        P("section", None),
        P("section", None),
        P("section", None, "tensor"),
        P("section", "tensor"),
        P("section", "tensor", None),
        P("section", None),
    )
    return jax.shard_map(
        on_line if fits_lines(mesh) else on_device,
        mesh=mesh,
        in_specs=placed,
        out_specs=(
            P("section", None, ("seq", "tensor"), None, None),
            P("section", None, ("seq", "tensor"), None, None),
            P("section", None),
            P("section", None),
            P("section", None, "seq", "tensor"),
            P("section", None, None),
            P("section", "tensor", "seq"),
            P("section", None),
            P("section", None),
            P("section", None),
            P("section", "seq", "tensor"),
            P("section", None),
            P("section", "tensor", "seq"),
            P("section", None),
        ),
        check_vma=False,
    )
```

```python
import functools
import types

import jax
import jax.numpy as jnp
from jax import lax
from jax.experimental import pallas as pl
from jax.experimental.pallas import tpu as pltpu
from jax.sharding import PartitionSpec as P

HDIM = 64
WIN = 64
QB = 64
KSEL = 64


NORM_EPS = 1e-05
MASKED = -1000000000.0


def from_behind(value, axis, steps):
    count = lax.axis_size(axis)
    first, last = (max(0, -steps), min(count, count - steps))
    return lax.ppermute(value, axis, [(source, source + steps) for source in range(first, last)])


def layer_norm(values, gain, shift):
    average = jnp.mean(values, axis=-1, keepdims=True)
    centred = values - average
    variance = jnp.mean(centred * centred, axis=-1, keepdims=True)
    return centred * lax.rsqrt(variance + NORM_EPS) * gain + shift


def gelu_tanh(values):
    return (
        0.5
        * values
        * (1.0 + jnp.tanh(0.7978845608028654 * (values + 0.044715 * values * values * values)))
    )


def gather_rows(row_block):
    return lax.all_gather(row_block, "tensor", axis=0, tiled=True)


def scatter_product(left_rows, weight, formula):
    return lax.psum_scatter(
        jnp.einsum(formula, left_rows, weight, preferred_element_type=jnp.float32).astype(
            jnp.bfloat16
        ),
        "tensor",
        scatter_dimension=0,
        tiled=True,
    ).astype(jnp.float32)


def near_slabs(full_rows, seq_start, seq_first, length_local):
    buckets = full_rows.shape[1]
    heads_local = full_rows.shape[2] // HDIM
    blocks = length_local // QB
    earlier = lax.dynamic_slice_in_dim(full_rows, jnp.maximum(seq_start - WIN, 0), WIN, 0)
    earlier = jnp.where(seq_first, jnp.zeros_like(earlier), earlier)
    local_part = lax.dynamic_slice_in_dim(full_rows, seq_start, length_local, 0)
    segment = jnp.concatenate([earlier, local_part], 0).reshape(
        length_local + WIN, buckets, heads_local, HDIM
    )
    return jnp.concatenate(
        [
            segment[offset_index * QB : offset_index * QB + length_local].reshape(
                blocks, QB, buckets, heads_local, HDIM
            )
            for offset_index in range(WIN // QB + 1)
        ],
        1,
    )


def far_rows(full_rows, flat_index):
    total_rows, buckets, feature_width = full_rows.shape
    heads_local = feature_width // HDIM
    return jnp.take(full_rows.reshape(total_rows * buckets * heads_local, HDIM), flat_index, axis=0)


def key_geometry(chosen_now, seq_start, blocks):
    buckets, heads_local = (chosen_now.shape[0], chosen_now.shape[1])
    bucket_ids = lax.broadcasted_iota(jnp.int32, chosen_now.shape, 0)
    head_ids = lax.broadcasted_iota(jnp.int32, chosen_now.shape, 1)
    flat_index = (chosen_now * buckets + bucket_ids) * heads_local + head_ids
    block_start = seq_start + QB * lax.broadcasted_iota(jnp.int32, (blocks, 1, 1), 0)
    query_ids = lax.broadcasted_iota(jnp.int32, (1, QB, 1), 1)
    key_ids = lax.broadcasted_iota(jnp.int32, (1, 1, WIN + QB), 2)
    distance = query_ids + WIN - key_ids
    near_ok = (distance >= 0) & (distance < WIN) & (block_start + key_ids - WIN >= 0)
    far_ok = chosen_now + WIN <= block_start.reshape(1, 1, blocks, 1)
    near_mask = jnp.broadcast_to(
        near_ok[:, None, None], (blocks, buckets, heads_local, QB, WIN + QB)
    )
    far_mask = jnp.broadcast_to(
        jnp.transpose(far_ok, (2, 0, 1, 3))[:, :, :, None, :],
        (blocks, buckets, heads_local, QB, KSEL),
    )
    return (flat_index, jnp.concatenate([near_mask, far_mask], -1))


def attention_setup(queries, key_rows, value_rows, chosen_now, seq_start, seq_first):
    length_local, buckets, feature_width = queries.shape
    heads_local = feature_width // HDIM
    blocks = length_local // QB
    query_blocks = queries.reshape(blocks, QB, buckets, heads_local, HDIM)
    flat_index, key_mask = key_geometry(chosen_now, seq_start, blocks)
    near_keys = near_slabs(key_rows, seq_start, seq_first, length_local)
    near_values = near_slabs(value_rows, seq_start, seq_first, length_local)
    far_keys = far_rows(key_rows, flat_index)
    far_values = far_rows(value_rows, flat_index)
    near_scores = jnp.einsum(
        "bqnhe,btnhe->bnhqt", query_blocks, near_keys, preferred_element_type=jnp.float32
    )
    far_scores = jnp.einsum(
        "bqnhe,nhbke->bnhqk", query_blocks, far_keys, preferred_element_type=jnp.float32
    )
    scores = jnp.where(
        key_mask, HDIM ** (-0.5) * jnp.concatenate([near_scores, far_scores], -1), MASKED
    )
    return (query_blocks, near_keys, near_values, far_keys, far_values, flat_index, scores)


def attend(queries, key_rows, value_rows, chosen_now, seq_start, seq_first):
    query_blocks, near_keys, near_values, far_keys, far_values, flat_index, scores = (
        attention_setup(queries, key_rows, value_rows, chosen_now, seq_start, seq_first)
    )
    span = WIN + QB
    row_top = jnp.max(scores, -1, keepdims=True)
    exp_terms = jnp.exp(scores - row_top)
    row_total = jnp.sum(exp_terms, -1, keepdims=True)
    softmax_low = (exp_terms / row_total).astype(jnp.bfloat16)
    near_part = jnp.einsum(
        "bnhqt,btnhe->bqnhe",
        softmax_low[..., :span],
        near_values,
        preferred_element_type=jnp.float32,
    )
    far_part = jnp.einsum(
        "bnhqk,nhbke->bqnhe",
        softmax_low[..., span:],
        far_values,
        preferred_element_type=jnp.float32,
    )
    return ((near_part + far_part).reshape(queries.shape), row_top + jnp.log(row_total))


def spread_back(near_grad, far_grad, flat_index, seq_start, seq_first, total_rows):
    blocks, span, buckets, heads_local, head_size = near_grad.shape
    length_local = blocks * QB
    feature_width = heads_local * head_size
    segment = jnp.zeros((length_local + WIN, buckets, heads_local, head_size), jnp.float32)
    for offset_index in range(WIN // QB + 1):
        piece = near_grad[:, offset_index * QB : (offset_index + 1) * QB].reshape(
            length_local, buckets, heads_local, head_size
        )
        segment = segment.at[offset_index * QB : offset_index * QB + length_local].add(piece)
    full_rows = jnp.zeros((total_rows * buckets * heads_local, head_size), jnp.float32)
    full_rows = full_rows.at[flat_index.reshape(-1)].add(far_grad.reshape(-1, head_size))
    full_rows = full_rows.reshape(total_rows, buckets, feature_width)
    local_part = segment[WIN:].reshape(length_local, buckets, feature_width)
    earlier = jnp.where(seq_first, 0.0, segment[:WIN].reshape(WIN, buckets, feature_width))
    full_rows = lax.dynamic_update_slice_in_dim(
        full_rows,
        lax.dynamic_slice_in_dim(full_rows, seq_start, length_local, 0) + local_part,
        seq_start,
        0,
    )
    earlier_start = jnp.maximum(seq_start - WIN, 0)
    full_rows = lax.dynamic_update_slice_in_dim(
        full_rows,
        lax.dynamic_slice_in_dim(full_rows, earlier_start, WIN, 0) + earlier,
        earlier_start,
        0,
    )
    return full_rows


def attend_back(
    queries, key_rows, value_rows, chosen_now, seq_start, seq_first, log_total, grad_mixed
):
    query_blocks, near_keys, near_values, far_keys, far_values, flat_index, scores = (
        attention_setup(queries, key_rows, value_rows, chosen_now, seq_start, seq_first)
    )
    span = WIN + QB
    score_scale = HDIM ** (-0.5)
    grad_blocks = grad_mixed.reshape(query_blocks.shape)
    weights_full = jnp.exp(scores - log_total)
    softmax_low = weights_full.astype(jnp.bfloat16)
    grad_near_weights = jnp.einsum(
        "bqnhe,btnhe->bnhqt", grad_blocks, near_values, preferred_element_type=jnp.float32
    )
    grad_far_weights = jnp.einsum(
        "bqnhe,nhbke->bnhqk", grad_blocks, far_values, preferred_element_type=jnp.float32
    )
    grad_weights = jnp.concatenate([grad_near_weights, grad_far_weights], -1)
    row_dot = jnp.sum(weights_full * grad_weights, -1, keepdims=True)
    grad_scores = (weights_full * (grad_weights - row_dot)).astype(jnp.bfloat16)
    grad_near, grad_far = (grad_scores[..., :span], grad_scores[..., span:])
    grad_queries = score_scale * (
        jnp.einsum("bnhqt,btnhe->bqnhe", grad_near, near_keys, preferred_element_type=jnp.float32)
        + jnp.einsum("bnhqk,nhbke->bqnhe", grad_far, far_keys, preferred_element_type=jnp.float32)
    )
    near_key_grad = score_scale * jnp.einsum(
        "bnhqt,bqnhe->btnhe", grad_near, query_blocks, preferred_element_type=jnp.float32
    )
    far_key_grad = score_scale * jnp.einsum(
        "bnhqk,bqnhe->nhbke", grad_far, query_blocks, preferred_element_type=jnp.float32
    )
    near_value_grad = jnp.einsum(
        "bnhqt,bqnhe->btnhe",
        softmax_low[..., :span],
        grad_blocks,
        preferred_element_type=jnp.float32,
    )
    far_value_grad = jnp.einsum(
        "bnhqk,bqnhe->nhbke",
        softmax_low[..., span:],
        grad_blocks,
        preferred_element_type=jnp.float32,
    )
    total_rows = key_rows.shape[0]
    key_grad = spread_back(
        near_key_grad, far_key_grad, flat_index, seq_start, seq_first, total_rows
    )
    value_grad = spread_back(
        near_value_grad, far_value_grad, flat_index, seq_start, seq_first, total_rows
    )
    return (grad_queries.reshape(queries.shape), key_grad, value_grad)


def forward_pass(hidden, params, chosen_now, query_mask, seq_start, seq_first, finish):
    (
        ln1_gain,
        ln1_shift,
        w_qkv,
        b_qv,
        w_out,
        b_out,
        ln2_gain,
        ln2_shift,
        w_fc,
        b_fc,
        w_proj,
        b_proj,
    ) = params
    hidden_wide = hidden.astype(jnp.float32)
    normed_all = gather_rows(layer_norm(hidden_wide, ln1_gain, ln1_shift).astype(jnp.bfloat16))
    projected = jnp.einsum("pnd,jdc->jpnc", normed_all, w_qkv, preferred_element_type=jnp.float32)
    queries = (projected[0] + b_qv[0]).astype(jnp.bfloat16)
    key_rows, value_rows = (
        lax.all_gather(projected[1].astype(jnp.bfloat16), "seq", axis=0, tiled=True),
        lax.all_gather((projected[2] + b_qv[1]).astype(jnp.bfloat16), "seq", axis=0, tiled=True),
    )
    attended, log_total = attend(queries, key_rows, value_rows, chosen_now, seq_start, seq_first)
    mixed_rows = (attended * query_mask[:, :, None]).astype(jnp.bfloat16)
    middle = hidden_wide + scatter_product(mixed_rows, w_out, "pnc,cd->pnd") + b_out
    normed_mlp = gather_rows(layer_norm(middle, ln2_gain, ln2_shift).astype(jnp.bfloat16))
    pre_active = (
        jnp.einsum("pnd,df->pnf", normed_mlp, w_fc, preferred_element_type=jnp.float32) + b_fc
    )
    active = gelu_tanh(pre_active).astype(jnp.bfloat16)
    if not finish:
        return (
            normed_all,
            queries,
            key_rows,
            value_rows,
            log_total,
            mixed_rows,
            middle,
            normed_mlp,
            pre_active,
            active,
        )
    output = (middle + scatter_product(active, w_proj, "pnf,fd->pnd") + b_proj).astype(jnp.bfloat16)
    return (output, (key_rows, value_rows))


def backward_pass(hidden, upstream, params, chosen_now, query_mask, seq_start, seq_first):
    (
        ln1_gain,
        ln1_shift,
        w_qkv,
        b_qv,
        w_out,
        b_out,
        ln2_gain,
        ln2_shift,
        w_fc,
        b_fc,
        w_proj,
        b_proj,
    ) = params
    (
        normed_all,
        queries,
        key_rows,
        value_rows,
        log_total,
        mixed_rows,
        middle,
        normed_mlp,
        pre_active,
        active,
    ) = forward_pass(hidden, params, chosen_now, query_mask, seq_start, seq_first, False)
    upstream_all = gather_rows(upstream)
    grad_w_proj = jnp.einsum(
        "pnf,pnd->fd", active, upstream_all, preferred_element_type=jnp.float32
    )
    grad_b_proj = jnp.sum(upstream.astype(jnp.float32), axis=(0, 1))
    grad_active = jnp.einsum(
        "pnd,fd->pnf", upstream_all, w_proj, preferred_element_type=jnp.float32
    )
    unused_value, gelu_pull = jax.vjp(gelu_tanh, pre_active)
    grad_pre = gelu_pull(grad_active)[0].astype(jnp.bfloat16)
    grad_w_fc = jnp.einsum("pnd,pnf->df", normed_mlp, grad_pre, preferred_element_type=jnp.float32)
    grad_b_fc = jnp.sum(grad_pre.astype(jnp.float32), axis=(0, 1))
    grad_normed_mlp = scatter_product(grad_pre, w_fc, "pnf,df->pnd")
    unused_norm, second_pull = jax.vjp(layer_norm, middle, ln2_gain, ln2_shift)
    grad_mid_norm, grad_ln2_gain, grad_ln2_shift = second_pull(grad_normed_mlp)
    grad_middle = upstream.astype(jnp.float32) + grad_mid_norm
    grad_branch = grad_middle.astype(jnp.bfloat16)
    grad_b_out = jnp.sum(grad_branch.astype(jnp.float32), axis=(0, 1))
    branch_all = gather_rows(grad_branch)
    grad_w_out = jnp.einsum(
        "pnc,pnd->cd", mixed_rows, branch_all, preferred_element_type=jnp.float32
    )
    grad_mixed = jnp.einsum(
        "pnd,cd->pnc", branch_all, w_out, preferred_element_type=jnp.float32
    ).astype(jnp.bfloat16) * query_mask[:, :, None].astype(jnp.bfloat16)
    grad_queries, key_grad_all, value_grad_all = attend_back(
        queries, key_rows, value_rows, chosen_now, seq_start, seq_first, log_total, grad_mixed
    )
    key_grad, value_grad = (
        lax.psum_scatter(
            key_grad_all.astype(jnp.bfloat16), "seq", scatter_dimension=0, tiled=True
        ).astype(jnp.float32),
        lax.psum_scatter(
            value_grad_all.astype(jnp.bfloat16), "seq", scatter_dimension=0, tiled=True
        ).astype(jnp.float32),
    )
    grad_project = jnp.stack(
        [
            grad_queries.astype(jnp.bfloat16),
            key_grad.astype(jnp.bfloat16),
            value_grad.astype(jnp.bfloat16),
        ],
        2,
    )
    grad_w_qkv = jnp.einsum(
        "pnd,pnjc->jdc", normed_all, grad_project, preferred_element_type=jnp.float32
    )
    grad_b_qv = jnp.sum(grad_project[:, :, 0::2].astype(jnp.float32), axis=(0, 1))
    grad_normed = scatter_product(grad_project, w_qkv, "pnjc,jdc->pnd")
    unused_first, first_pull = jax.vjp(layer_norm, hidden.astype(jnp.float32), ln1_gain, ln1_shift)
    grad_in_norm, grad_ln1_gain, grad_ln1_shift = first_pull(grad_normed)
    grad_hidden = (grad_middle + grad_in_norm).astype(jnp.bfloat16)
    block_grads = (
        grad_ln1_gain,
        grad_ln1_shift,
        grad_w_qkv,
        grad_b_qv,
        grad_w_out,
        grad_b_out,
        grad_ln2_gain,
        grad_ln2_shift,
        grad_w_fc,
        grad_b_fc,
        grad_w_proj,
        grad_b_proj,
    )
    return (grad_hidden, block_grads)


def on_device(
    inputs,
    cotangent,
    lengths,
    chosen,
    ln1_gain,
    ln1_shift,
    w_qkv,
    b_qv,
    w_out,
    b_out,
    ln2_gain,
    ln2_shift,
    w_fc,
    b_fc,
    w_proj,
    b_proj,
):
    params = tuple(
        (
            weight_array[0]
            for weight_array in (
                ln1_gain,
                ln1_shift,
                w_qkv,
                b_qv,
                w_out,
                b_out,
                ln2_gain,
                ln2_shift,
                w_fc,
                b_fc,
                w_proj,
                b_proj,
            )
        )
    )
    section_index = lax.axis_index("section")
    section_count = lax.axis_size("section")
    seq_index = lax.axis_index("seq")
    tensor_index = lax.axis_index("tensor")
    tensor_count = lax.axis_size("tensor")
    micro_count, rows_local, buckets, feature_width = inputs.shape
    length_local = rows_local * tensor_count
    heads_width = w_qkv.shape[-1]
    seq_start = seq_index * length_local
    seq_first = seq_index == 0
    positions = seq_start + lax.broadcasted_iota(jnp.int32, (micro_count, length_local, buckets), 1)
    mask_all = (positions < lengths[:, None, :]).astype(jnp.float32)
    mask_rows = lax.dynamic_slice_in_dim(mask_all, tensor_index * rows_local, rows_local, 1)
    step_count = micro_count + section_count - 1
    chosen_section = chosen[0]
    received = jnp.zeros((rows_local, buckets, feature_width), jnp.bfloat16)
    stored = jnp.zeros((micro_count, rows_local, buckets, feature_width), jnp.bfloat16)
    outputs = jnp.zeros_like(stored)
    for step_index in range(step_count):
        micro_index = step_index - section_index
        running = (micro_index >= 0) & (micro_index < micro_count)
        slot_index = jnp.clip(micro_index, 0, micro_count - 1)
        block_in = jnp.where(
            section_index == 0, lax.dynamic_index_in_dim(inputs, slot_index, 0, False), received
        )
        chosen_now = lax.dynamic_index_in_dim(chosen_section, slot_index, 0, False)
        query_mask = lax.dynamic_index_in_dim(mask_all, slot_index, 0, False)
        result, key_pair = forward_pass(
            block_in, params, chosen_now, query_mask, seq_start, seq_first, True
        )
        stored = jnp.where(
            running, lax.dynamic_update_index_in_dim(stored, block_in, slot_index, 0), stored
        )
        outputs = jnp.where(
            running, lax.dynamic_update_index_in_dim(outputs, result, slot_index, 0), outputs
        )
        received = from_behind(result, "section", 1)
    back_received = jnp.zeros((rows_local, buckets, feature_width), jnp.bfloat16)
    in_grads = jnp.zeros_like(stored)
    totals = None
    for step_index in range(step_count):
        micro_index = step_index - (section_count - 1 - section_index)
        running = (micro_index >= 0) & (micro_index < micro_count)
        slot_index = jnp.clip(micro_index, 0, micro_count - 1)
        chosen_now = lax.dynamic_index_in_dim(chosen_section, slot_index, 0, False)
        query_mask = lax.dynamic_index_in_dim(mask_all, slot_index, 0, False)
        local_mask = lax.dynamic_index_in_dim(mask_rows, slot_index, 0, False)
        top_grad = (
            lax.dynamic_index_in_dim(cotangent, slot_index, 0, False).astype(jnp.float32)
            * local_mask[:, :, None]
        ).astype(jnp.bfloat16)
        upstream = jnp.where(section_index == section_count - 1, top_grad, back_received)
        hidden = lax.dynamic_index_in_dim(stored, slot_index, 0, False)
        grad_hidden, block_grads = backward_pass(
            hidden, upstream, params, chosen_now, query_mask, seq_start, seq_first
        )
        block_grads = tuple(
            (jnp.where(running, grad_part, jnp.zeros_like(grad_part)) for grad_part in block_grads)
        )
        totals = (
            block_grads
            if step_index == 0
            else tuple(
                (total_part + grad_part for total_part, grad_part in zip(totals, block_grads))
            )
        )
        in_grads = jnp.where(
            running, lax.dynamic_update_index_in_dim(in_grads, grad_hidden, slot_index, 0), in_grads
        )
        back_received = from_behind(grad_hidden, "section", -1)
    (
        sum_ln1_gain,
        sum_ln1_shift,
        sum_w_qkv,
        sum_b_qv,
        sum_w_out,
        sum_b_out,
        sum_ln2_gain,
        sum_ln2_shift,
        sum_w_fc,
        sum_b_fc,
        sum_w_proj,
        sum_b_proj,
    ) = totals
    part_qkv, part_out, part_fc, part_proj = (
        lax.psum_scatter(
            sum_w_qkv.astype(jnp.bfloat16), "seq", scatter_dimension=1, tiled=True
        ).astype(jnp.float32),
        lax.psum_scatter(
            sum_w_out.astype(jnp.bfloat16), "seq", scatter_dimension=1, tiled=True
        ).astype(jnp.float32),
        lax.psum_scatter(
            sum_w_fc.astype(jnp.bfloat16), "seq", scatter_dimension=0, tiled=True
        ).astype(jnp.float32),
        lax.psum_scatter(
            sum_w_proj.astype(jnp.bfloat16), "seq", scatter_dimension=1, tiled=True
        ).astype(jnp.float32),
    )
    bias_qv = lax.dynamic_update_slice_in_dim(
        jnp.zeros((2, feature_width), jnp.float32), sum_b_qv, tensor_index * heads_width, 1
    )
    units_local = sum_b_fc.shape[0]
    bias_fc = lax.dynamic_update_slice_in_dim(
        jnp.zeros((units_local * tensor_count,), jnp.float32),
        sum_b_fc,
        tensor_index * units_local,
        0,
    )
    small_sums = lax.psum(
        (
            sum_ln1_gain,
            sum_ln1_shift,
            bias_qv,
            sum_b_out,
            sum_ln2_gain,
            sum_ln2_shift,
            bias_fc,
            sum_b_proj,
        ),
        ("seq", "tensor"),
    )
    return (
        outputs[None],
        in_grads[None],
        small_sums[0][None],
        small_sums[1][None],
        part_qkv[None],
        small_sums[2][None],
        part_out[None],
        small_sums[3][None],
        small_sums[4][None],
        small_sums[5][None],
        part_fc[None],
        small_sums[6][None],
        part_proj[None],
        small_sums[7][None],
    )


STREAMS = 2
NRM, NMLP, UPS, BRN, ACT, GPRE, MIX, DQKV = range(8)
F32 = jnp.float32
LOW = jnp.bfloat16
MESH_ID = pl.DeviceIdType.MESH


def dot_nn(left, right):
    return lax.dot_general(left, right, (((1,), (0,)), ((), ())), preferred_element_type=F32)


def dot_nt(left, right):
    return lax.dot_general(left, right, (((1,), (1,)), ((), ())), preferred_element_type=F32)


def dot_tn(left, right):
    return lax.dot_general(left, right, (((0,), (0,)), ((), ())), preferred_element_type=F32)


def standard(rows):
    centred = rows - jnp.mean(rows, axis=-1, keepdims=True)
    scale = lax.rsqrt(jnp.mean(centred * centred, axis=-1, keepdims=True) + NORM_EPS)
    return centred * scale, scale


def standard_back(grad, xhat, scale):
    inner = jnp.mean(grad * xhat, axis=-1, keepdims=True)
    return scale * (grad - jnp.mean(grad, axis=-1, keepdims=True) - xhat * inner)


def column_sum(rows):
    return jnp.sum(rows.astype(F32), axis=0, keepdims=True)


def relay_kernel(names, *refs):
    r = types.SimpleNamespace(**dict(zip(names, refs)))
    a, c, t = (lax.axis_index(name) for name in ("section", "seq", "tensor"))
    lines = lax.axis_size("section")
    chips = lax.axis_size("tensor")
    rows, buckets, width = r.inputs.shape[1:]
    half_width = width // 2
    local = rows * chips
    total = 2 * local
    sub = rows // STREAMS
    stream_rows = local // STREAMS
    head_width = r.wo_in.shape[0]
    heads = head_width // HDIM
    blocks = local // QB
    units = r.wp_in.shape[0]
    scale = HDIM ** (-0.5)
    streams = range(STREAMS)

    def remote(src, dst, send, recv, **target):
        return pltpu.make_async_remote_copy(
            src_ref=src,
            dst_ref=dst,
            send_sem=send,
            recv_sem=recv,
            device_id=target,
            device_id_type=MESH_ID,
        )

    def drain(ref, sem):
        pltpu.make_async_copy(ref, ref, sem).wait()

    def row_block(index, size):
        return pl.ds(pl.multiple_of(index * size, size), size)

    mine = row_block(t, sub)
    my_half = row_block(c, local)

    barrier = pltpu.get_barrier_semaphore()
    for core in range(2):
        for step in range(1, chips):
            there = {"tensor": (t + step) % chips, "seq": core}
            pl.semaphore_signal(barrier, inc=1, device_id=there, device_id_type=MESH_ID)
        for step in range(1, lines):
            there = {"section": (a + step) % lines, "seq": core}
            pl.semaphore_signal(barrier, inc=1, device_id=there, device_id_type=MESH_ID)
    pl.semaphore_signal(barrier, inc=1, device_id={"seq": 1 - c}, device_id_type=MESH_ID)
    pl.semaphore_wait(barrier, 2 * (chips - 1) + 2 * (lines - 1) + 1)

    def beside(s):
        return s + 1 - 2 * (s % 2)

    def above(s):
        return (s + 2) % 4

    def store(p):
        return (r.wq, r.wo, r.wf, r.wp)[p]

    def source(p):
        return (r.wq_in, r.wo_in, r.wf_in, r.wp_in)[p]

    def height(p):
        return source(p).shape[0]

    def core_half(p, s, core):
        return store(p).at[s, row_block(core, height(p) // 2)]

    def first_hop(p, s, neighbour, which):
        return remote(
            source(p).at[row_block(c, height(p) // 2)],
            core_half(p, s, c),
            r.w_first_s.at[p, which],
            r.w_first_r.at[s, p],
            section=neighbour,
        )

    def second_hop(p, s, which):
        view = store(p).at[s, row_block(2 * c + which, height(p) // 4)]
        return remote(
            view, view, r.w_second_s.at[s, p], r.w_second_r.at[s, p, which], section=3 - s
        )

    def core_hop(p, s, core):
        view = core_half(p, s, core)
        return remote(view, view, r.w_core_s.at[s, p], r.w_core_r.at[s, p], seq=1 - c)

    def own_copy(p):
        return pltpu.make_async_copy(source(p), store(p).at[a], r.w_own.at[p])

    def pass_on(s, p, which):
        line = (beside(s), above(s))[which]

        @pl.when(a == line)
        def _():
            first_hop(p, s, line, which).wait_recv()
            second_hop(p, s, which).start()
            core_hop(p, s, c).start()

    def pass_later(pieces, at_first):
        for later in range(1, lines):
            for which in range(2):
                if ((beside(later), above(later))[which] == 0) == at_first:
                    for p in pieces:
                        pass_on(later, p, which)

    def pass_far(s, p):
        @pl.when(a == 3 - s)
        def _():
            second_hop(p, s, 0).wait_recv()
            second_hop(p, s, 1).wait_recv()
            core_hop(p, s, c).start()

    def need(s, p):
        @pl.when(s == 0)
        def _():
            pass_on(0, p, 0)
            pass_on(0, p, 1)
            pass_far(0, p)

        @pl.when(a == s)
        def _():
            own_copy(p).wait()

        @pl.when(a != s)
        def _():
            core_hop(p, s, 1 - c).wait_recv()

    def small_copy(step, line, slot):
        return remote(
            r.small_own, r.small.at[slot], r.small_s.at[step], r.small_r.at[slot], section=line
        )

    def count_copy(step, line, slot):
        return remote(
            r.count_own.at[line],
            r.count.at[slot],
            r.count_s.at[step],
            r.count_r.at[slot],
            section=line,
        )

    singles = (r.ln1_gain, r.ln1_shift, r.ln2_gain, r.ln2_shift, r.b_out, r.b_proj)
    for place, single in enumerate(singles):
        r.small_own[place : place + 1] = single[...]
    r.small_own[6:7, :units] = r.b_fc[...]
    r.small_own[7:8, :head_width] = r.b_qv[0:1]
    r.small_own[7:8, half_width : half_width + head_width] = r.b_qv[1:2]
    for step in range(1, lines):
        small_copy(step - 1, (a + step) % lines, a).start()
    for p in range(4):
        for which, line in enumerate((beside(a), above(a))):
            first_hop(p, a, line, which).start()
    for p in range(4):
        own_copy(p).start()
    r.small[a] = r.small_own[...]

    def place_of(index):
        inside = index % local
        stream, left = inside // stream_rows, inside % stream_rows
        return (index // local) * local + (left // sub) * rows + stream * sub + left % sub

    def iota(shape, dimension):
        return lax.broadcasted_iota(jnp.int32, shape, dimension)

    square = jnp.where(iota((KSEL, KSEL), 0) == iota((KSEL, KSEL), 1), 1.0, 0.0).astype(LOW)
    position = place_of(iota((KSEL, total), 1)).astype(F32)
    for pair in range(lines * heads):
        line, head = pair // heads, pair % heads
        columns = dot_nt(square, r.chosen[pair].astype(F32).astype(LOW))
        for block in range(blocks):
            pick = head * blocks + block
            r.count_own[line, pick : pick + 1, :] = jnp.sum(
                jnp.where(columns[:, block : block + 1] == position, 1.0, 0.0),
                axis=0,
                keepdims=True,
            )
    for step in range(1, lines):
        count_copy(step - 1, (a + step) % lines, a).start()
    r.count[a] = r.count_own[a]

    partners = (3 - t, (t + 2) % 4, t + 1 - 2 * (t % 2))

    def gather(buffer, s, kind, j, slot, chip):
        view = buffer.at[s, j, row_block(chip, sub)]
        return remote(
            view,
            view,
            r.ag_s.at[kind, j, slot],
            r.ag_r.at[kind, j, slot],
            tensor=partners[slot],
        )

    def gather_start(buffer, s, kind, j):
        for slot in range(chips - 1):
            gather(buffer, s, kind, j, slot, t).start()

    def gather_wait(buffer, s, kind, j):
        for slot in range(chips - 1):
            gather(buffer, s, kind, j, slot, partners[slot]).wait_recv()
        for slot in range(chips - 1):
            gather(buffer, s, kind, j, slot, t).wait_send()

    def scatter(s, kind, j, slot):
        return remote(
            r.part.at[kind, j, row_block(partners[slot], sub)],
            r.arrived.at[s, kind, j, slot],
            r.rs_s.at[kind, j, slot],
            r.rs_r.at[kind, j, slot],
            tensor=partners[slot],
        )

    def scatter_start(s, kind, j, product):
        r.part[kind, j] = product.astype(LOW)
        for slot in range(chips - 1):
            scatter(s, kind, j, slot).start()

    def scatter_sum(s, kind, j):
        result = r.part[kind, j, mine].astype(F32)
        for slot in range(chips - 1):
            scatter(s, kind, j, slot).wait_recv()
            result = result + r.arrived[s, kind, j, slot].astype(F32)
        for slot in range(chips - 1):
            scatter(s, kind, j, slot).wait_send()
        return result

    own_rows = (r.nrm, r.nmlp, r.ups, r.brn, r.act, r.gpre, r.mix, r.dqkv)
    all_rows = (
        r.all_nrm,
        r.all_nmlp,
        r.all_ups,
        r.all_brn,
        r.all_act,
        r.all_gpre,
        r.all_mix,
        r.all_dqkv,
    )

    def rows_copy(index, s, same, stays=False):
        core = c if same else 1 - c
        src = own_rows[index].at[s]
        dst = all_rows[index].at[a, c]
        if index <= BRN:
            src = src.at[:, :, row_block(core, half_width)]
        recv = r.rows_r.at[index]
        if stays:
            return pltpu.make_async_copy(src, dst, recv)
        if same:
            return remote(src, dst, r.rows_s.at[index, s, 0], recv, section=s)
        return remote(src, dst, r.rows_s.at[index, s, 1], recv, section=s, seq=1 - c)

    def rows_start(index, s):
        @pl.when(a == s)
        def _():
            rows_copy(index, s, True, True).start()

        @pl.when(a != s)
        def _():
            rows_copy(index, s, True).start()

        if index <= BRN:
            rows_copy(index, s, False).start()

    def rows_sent(index, s):
        @pl.when(a != s)
        def _():
            rows_copy(index, s, True).wait_send()

        if index <= BRN:
            rows_copy(index, s, False).wait_send()

    def share_copy(index, core):
        view = all_rows[index].at[:, core]
        return remote(view, view, r.share_s.at[index - ACT], r.share_r.at[index - ACT], seq=1 - c)

    def share(index):
        drain(all_rows[index].at[:, c], r.rows_r.at[index])
        share_copy(index, c).start()

    def home_copy(src, dst, send, recv, s):
        return remote(src.at[s], dst.at[a], send.at[s], recv, section=s)

    def home_start(src, dst, send, recv, s):
        @pl.when(a == s)
        def _():
            pltpu.make_async_copy(src.at[s], dst.at[a], recv).start()

        @pl.when(a != s)
        def _():
            home_copy(src, dst, send, recv, s).start()

    def home_sent(*what):
        @pl.when(a != what[-1])
        def _():
            home_copy(*what).wait_send()

    out_home = (r.out_low, r.acts, r.out_s, r.out_r)
    grad_home = (r.grad_low, r.grads, r.grad_s, r.grad_r)
    norm_home = (r.norm_part, r.norm_all, r.norm_s, r.norm_r)

    length = r.lengths[a // buckets, a % buckets]
    query = place_of(c * local + iota((local, total), 0))
    key = place_of(iota((local, total), 1))
    near = jnp.where((query >= key) & (query - key < WIN), 1.0, 0.0)
    key_row = place_of(iota((1, total), 1))
    block_of = place_of(iota((local, total), 0)) // QB
    first_block = jnp.where(block_of == 0, 1.0, 0.0)

    def row_mask(place):
        return jnp.where(place < length, 1.0, 0.0)

    def multiplicity(s, head):
        times = near
        for block in range(blocks):
            pick = head * blocks + block
            limit = (c * blocks + block) * QB - WIN
            counted = jnp.where(key_row <= limit, r.count[s, pick : pick + 1, :], 0.0)
            times = times + jnp.where(block_of == block, counted, 0.0)
        return times

    def head_cols(head):
        return slice(head * HDIM, (head + 1) * HDIM)

    def kv_copy(s, core):
        view = r.kv.at[s, :, row_block(core, local)]
        return remote(view, view, r.kv_s.at[s], r.kv_r.at[s], seq=1 - c)

    def dkv_copy(s):
        return remote(r.dkv_out.at[s], r.dkv_in.at[s], r.dkv_s.at[s], r.dkv_r.at[s], seq=1 - c)

    def flat(array):
        return array.reshape(local, array.shape[-1])

    def own_sequence(ref):
        both = ref[a // buckets].astype(F32)
        picked = both[:, 0, :]
        for bucket in range(1, buckets):
            picked = jnp.where(a % buckets == bucket, both[:, bucket, :], picked)
        return picked

    def part_rows(j):
        return slice(j * sub, (j + 1) * sub)

    r.hidden[...] = own_sequence(r.inputs)
    own_place = c * local + t * rows + iota((rows, 1), 0)
    r.upstream[...] = (own_sequence(r.cotangent) * row_mask(own_place)).astype(LOW)
    r.norm_part[...] = jnp.zeros_like(r.norm_part)

    def enter(s, j):
        xhat, inverse = standard(r.hidden[part_rows(j)])
        r.xhat1[s, j] = xhat
        r.inv1[s, j] = jnp.broadcast_to(inverse, (sub, 128))
        r.nrm[s, j, mine] = (xhat * r.small[s, 0:1] + r.small[s, 1:2]).astype(LOW)
        gather_start(r.nrm, s, 0, j)

    def project(s, j):
        gather_wait(r.nrm, s, 0, j)
        normed = r.nrm[s, j]
        place = row_block(c * STREAMS + j, stream_rows)
        bias_v = r.small[s, 7:8, half_width : half_width + head_width]
        key_rows = dot_nt(normed, r.wq[s, head_width : 2 * head_width])
        value_rows = dot_nt(normed, r.wq[s, 2 * head_width : 3 * head_width]) + bias_v
        r.kv[s, 0, place] = key_rows.astype(LOW)
        r.kv[s, 1, place] = value_rows.astype(LOW)

    def ask(s, j):
        queries = dot_nt(r.nrm[s, j], r.wq[s, 0:head_width]) + r.small[s, 7:8, :head_width]
        r.qry[s, j] = queries.astype(LOW)

    def attend_line(s):
        mixed = []
        queries = flat(r.qry[s])
        for head in range(heads):
            times = multiplicity(s, head)
            scores = scale * dot_nt(queries[:, head_cols(head)], r.kv[s, 0, :, head_cols(head)])
            scores = jnp.where(times > 0.0, scores, MASKED)
            top = jnp.max(scores, axis=-1, keepdims=True)
            terms = times * jnp.exp(scores - top)
            weights = terms / jnp.sum(terms, axis=-1, keepdims=True)
            r.soft[s, head] = weights
            mixed.append(dot_nn(weights.astype(LOW), r.kv[s, 1, :, head_cols(head)]))
        mask = row_mask(place_of(c * local + iota((local, 1), 0)))
        mixed = (jnp.concatenate(mixed, axis=-1) * mask).astype(LOW)
        r.mix[s] = mixed.reshape(r.mix.shape[1:])

    def leave_attention(s, j):
        scatter_start(s, 0, j, dot_nn(r.mix[s, j], r.wo[s]))

    def between(s, j):
        middle = r.hidden[part_rows(j)] + scatter_sum(s, 0, j) + r.small[s, 4:5]
        r.middle[part_rows(j)] = middle
        xhat, inverse = standard(middle)
        r.xhat2[s, j] = xhat
        r.inv2[s, j] = jnp.broadcast_to(inverse, (sub, 128))
        r.nmlp[s, j, mine] = (xhat * r.small[s, 2:3] + r.small[s, 3:4]).astype(LOW)
        gather_start(r.nmlp, s, 1, j)

    def feed(s, j):
        gather_wait(r.nmlp, s, 1, j)
        before = dot_nn(r.nmlp[s, j], r.wf[s]) + r.small[s, 6:7, :units]
        bend = jnp.tanh(0.7978845608028654 * (before + 0.044715 * before * before * before))
        r.act[s, j] = (0.5 * before * (1.0 + bend)).astype(LOW)
        r.slope[s, j] = 0.5 * (1.0 + bend) + 0.5 * before * (1.0 - bend * bend) * (
            0.7978845608028654 * (1.0 + 3 * 0.044715 * before * before)
        )

    def leave_feed(s, j):
        scatter_start(s, 1, j, dot_nn(r.act[s, j], r.wp[s]))

    def finish(s, j):
        result = r.middle[part_rows(j)] + scatter_sum(s, 1, j) + r.small[s, 5:6]
        r.out_low[s, part_rows(j)] = result.astype(LOW)
        r.hidden[part_rows(j)] = result.astype(LOW).astype(F32)

    def small_ready(s):
        @pl.when(a != s)
        def _():
            small_copy(0, a, s).wait_recv()

    small_ready(0)
    for j in streams:
        enter(0, j)

    def forward(s, _):
        need(s, 0)
        for j in streams:
            project(s, j)
        kv_copy(s, c).start()
        for j in streams:
            ask(s, j)
        rows_start(NRM, s)

        @pl.when(a != s)
        def _():
            count_copy(0, a, s).wait_recv()

        kv_copy(s, 1 - c).wait_recv()
        attend_line(s)
        need(s, 1)
        for j in streams:
            leave_attention(s, j)
        rows_start(MIX, s)

        @pl.when(s == 0)
        def _():
            pass_later((0, 1), False)

        @pl.when(s > 0)
        def _():
            pass_far(s, 2)
            pass_far(s, 3)

        for j in streams:
            between(s, j)
        need(s, 2)

        @pl.when(s == 0)
        def _():
            pass_later((2,), False)

        for j in streams:
            feed(s, j)
            if j == 0:
                need(s, 3)
            leave_feed(s, j)

        @pl.when(s == 0)
        def _():
            pass_later((3,), False)

        rows_start(NMLP, s)
        rows_start(ACT, s)

        @pl.when(s + 1 < lines)
        def _():
            small_ready(s + 1)

        for j in streams:
            finish(s, j)

            @pl.when(s + 1 < lines)
            def _():
                enter(s + 1, j)

        home_start(*out_home, s)

        @pl.when(s == 0)
        def _():
            pass_later(range(4), True)

        @pl.when(s + 1 < lines)
        def _():
            pass_far(s + 1, 0)
            pass_far(s + 1, 1)

        return 0

    lax.fori_loop(0, lines, forward, 0)

    def turn(s, j):
        upstream = r.upstream[part_rows(j)]
        r.ups[s, j, mine] = upstream
        gather_start(r.ups, s, 2, j)
        r.norm_part[s, 5:6] += column_sum(upstream)

    def feed_back(s, j):
        gather_wait(r.ups, s, 2, j)
        grad_pre = (dot_nt(r.ups[s, j], r.wp[s]) * r.slope[s, j]).astype(LOW)
        r.gpre[s, j] = grad_pre
        scatter_start(s, 2, j, dot_nt(grad_pre, r.wf[s]))
        r.norm_part[s, 6:7, :units] += column_sum(grad_pre)

    def between_back(s, j):
        grad = scatter_sum(s, 2, j)
        xhat = r.xhat2[s, j]
        upstream = r.upstream[part_rows(j)].astype(F32)
        grad_middle = upstream + standard_back(
            grad * r.small[s, 2:3], xhat, r.inv2[s, j, :, 0:1]
        )
        r.middle[part_rows(j)] = grad_middle
        branch = grad_middle.astype(LOW)
        r.brn[s, j, mine] = branch
        gather_start(r.brn, s, 3, j)
        r.norm_part[s, 2:3] += column_sum(grad * xhat)
        r.norm_part[s, 3:4] += column_sum(grad)
        r.norm_part[s, 4:5] += column_sum(branch)

    def mixed_back(s, j):
        gather_wait(r.brn, s, 3, j)
        place = place_of(c * local + j * stream_rows + iota((stream_rows, 1), 0))
        r.gmix[j] = (dot_nt(r.brn[s, j], r.wo[s]) * row_mask(place)).astype(LOW)

    def attend_line_back(s):
        grad_q, grad_k, grad_v = [], [], []
        grad_mixed = flat(r.gmix[...])
        queries = flat(r.qry[s])
        for head in range(heads):
            cols = head_cols(head)
            weights = r.soft[s, head]
            grad_head = grad_mixed[:, cols]
            grad_weights = dot_nt(grad_head, r.kv[s, 1, :, cols])
            inner = jnp.sum(weights * grad_weights, axis=-1, keepdims=True)
            grad_scores = (weights * (grad_weights - inner)).astype(LOW)
            grad_k.append(scale * dot_tn(grad_scores, queries[:, cols]))
            grad_v.append(dot_tn(weights.astype(LOW), grad_head))
            grad_q.append(scale * dot_nn(grad_scores, r.kv[s, 0, :, cols]))
        r.dkv_all[0] = jnp.concatenate(grad_k, axis=-1)
        r.dkv_all[1] = jnp.concatenate(grad_v, axis=-1)
        r.dkv_out[s] = r.dkv_all[:, row_block(1 - c, local)].astype(LOW)
        dkv_copy(s).start()
        grad_q = jnp.concatenate(grad_q, axis=-1).astype(LOW)
        r.dqkv[s, 0] = grad_q.reshape(r.dqkv.shape[2:])
        r.norm_part[s, 7:8, :head_width] = column_sum(grad_q)
        dkv_copy(s).wait_recv()
        for which in range(2):
            joined = r.dkv_all[which, my_half] + r.dkv_in[s, which].astype(F32)
            joined = joined.astype(LOW)
            r.dqkv[s, 1 + which] = joined.reshape(r.dqkv.shape[2:])
            if which == 1:
                r.norm_part[s, 7:8, half_width : half_width + head_width] = column_sum(joined)

    def leave_back(s, j):
        product = dot_nn(r.dqkv[s, 0, j], r.wq[s, 0:head_width])
        for which in range(1, 3):
            weight = r.wq[s, which * head_width : (which + 1) * head_width]
            product = product + dot_nn(r.dqkv[s, which, j], weight)
        scatter_start(s, 3, j, product)

    def finish_back(s, j):
        grad = scatter_sum(s, 3, j)
        xhat = r.xhat1[s, j]
        result = r.middle[part_rows(j)] + standard_back(
            grad * r.small[s, 0:1], xhat, r.inv1[s, j, :, 0:1]
        )
        r.upstream[part_rows(j)] = result.astype(LOW)
        r.grad_low[s, part_rows(j)] = result.astype(LOW)
        r.norm_part[s, 0:1] += column_sum(grad * xhat)
        r.norm_part[s, 1:2] += column_sum(grad)

    for j in streams:
        turn(lines - 1, j)

    def backward(index, _):
        s = lines - 1 - index
        for j in streams:
            feed_back(s, j)
        rows_start(UPS, s)
        rows_start(GPRE, s)

        @pl.when(index == 1)
        def _():
            share(ACT)
            share(MIX)

        for j in streams:
            between_back(s, j)
        for j in streams:
            mixed_back(s, j)
        rows_start(BRN, s)
        attend_line_back(s)
        for j in streams:
            leave_back(s, j)
        rows_start(DQKV, s)
        for j in streams:
            finish_back(s, j)

            @pl.when(s > 0)
            def _():
                turn(s - 1, j)

        home_start(*norm_home, s)
        home_start(*grad_home, s)
        return 0

    lax.fori_loop(0, lines, backward, 0)

    share(GPRE)
    share(DQKV)

    drain(r.norm_all, r.norm_r)
    slot = c * chips + t
    norm_sum = r.norm_all[0]
    for line in range(1, lines):
        norm_sum = norm_sum + r.norm_all[line]
    r.ends[slot] = norm_sum

    def ends_copy(step):
        core, chip = step // chips, step % chips
        view = r.ends.at[slot]
        return remote(
            view,
            view,
            r.ends_s.at[step - 1],
            r.ends_r,
            seq=(c + core) % 2,
            tensor=(t + chip) % chips,
        )

    for step in range(1, 2 * chips):
        ends_copy(step).start()

    for index in range(ACT):
        drain(all_rows[index], r.rows_r.at[index])
    for index in range(ACT, 8):
        share_copy(index, 1 - c).wait_recv()
        share_copy(index, c).wait_send()
    drain(r.acts, r.out_r)
    drain(r.grads, r.grad_r)
    drain(r.ends.at[0 : 2 * chips - 1], r.ends_r)
    for step in range(1, 2 * chips):
        ends_copy(step).wait_send()
    for step in range(1, lines):
        small_copy(step - 1, (a + step) % lines, a).wait_send()
        count_copy(step - 1, (a + step) % lines, a).wait_send()
    for p in range(4):
        for which, line in enumerate((beside(a), above(a))):
            first_hop(p, a, line, which).wait_send()

    def sent(s, _):
        home_sent(*out_home, s)
        home_sent(*grad_home, s)
        home_sent(*norm_home, s)
        kv_copy(s, c).wait_send()
        dkv_copy(s).wait_send()
        for index in range(8):
            rows_sent(index, s)
        for p in range(4):

            @pl.when((a == beside(s)) | (a == above(s)))
            def _():
                second_hop(p, s, 0).wait_send()

            @pl.when(a != s)
            def _():
                core_hop(p, s, c).wait_send()

        return 0

    lax.fori_loop(0, lines, sent, 0)


def relay_call(inputs, cotangent, lengths, chosen, singles, weights):
    lines = lax.axis_size("section")
    chips = lax.axis_size("tensor")
    rows, buckets, width = inputs.shape[1:]
    local, total, half = rows * chips, 2 * rows * chips, width // 2
    head_width, units = weights["wo_in"].shape[0], weights["wp_in"].shape[0]
    heads = head_width // HDIM
    sub, stream = rows // STREAMS, local // STREAMS
    peers = chips - 1
    vmem, dma = pltpu.VMEM, pltpu.SemaphoreType.DMA
    operands = dict(
        inputs=inputs,
        cotangent=cotangent,
        lengths=lengths,
        chosen=chosen,
        **singles,
        **weights,
    )

    def space(name):
        if name in weights:
            return pl.ANY
        return pltpu.SMEM if operands[name] is lengths else pltpu.VMEM

    sums = dict(
        acts=((lines, rows, width), LOW),
        grads=((lines, rows, width), LOW),
        ends=((2 * chips, 8, width), F32),
    )
    gathered = dict(
        all_nrm=((lines, 2, STREAMS, stream, half), LOW),
        all_nmlp=((lines, 2, STREAMS, stream, half), LOW),
        all_ups=((lines, 2, STREAMS, stream, half), LOW),
        all_brn=((lines, 2, STREAMS, stream, half), LOW),
        all_act=((lines, 2, STREAMS, stream, units), LOW),
        all_gpre=((lines, 2, STREAMS, stream, units), LOW),
        all_mix=((lines, 2, STREAMS, stream, head_width), LOW),
        all_dqkv=((lines, 2, 3, STREAMS, stream, head_width), LOW),
    )
    outputs = dict(**sums, **gathered)
    scratch = dict(
        wq=vmem((lines,) + weights["wq_in"].shape, LOW),
        wo=vmem((lines,) + weights["wo_in"].shape, LOW),
        wf=vmem((lines,) + weights["wf_in"].shape, LOW),
        wp=vmem((lines,) + weights["wp_in"].shape, LOW),
        small_own=vmem((8, width), F32),
        small=vmem((lines, 8, width), F32),
        count_own=vmem((lines, 8, total), F32),
        count=vmem((lines, 8, total), F32),
        hidden=vmem((rows, width), F32),
        middle=vmem((rows, width), F32),
        upstream=vmem((rows, width), LOW),
        xhat1=vmem((lines, STREAMS, sub, width), F32),
        inv1=vmem((lines, STREAMS, sub, 128), F32),
        xhat2=vmem((lines, STREAMS, sub, width), F32),
        inv2=vmem((lines, STREAMS, sub, 128), F32),
        nrm=vmem((lines, STREAMS, stream, width), LOW),
        nmlp=vmem((lines, STREAMS, stream, width), LOW),
        ups=vmem((lines, STREAMS, stream, width), LOW),
        brn=vmem((lines, STREAMS, stream, width), LOW),
        act=vmem((lines, STREAMS, stream, units), LOW),
        gpre=vmem((lines, STREAMS, stream, units), LOW),
        slope=vmem((lines, STREAMS, stream, units), F32),
        mix=vmem((lines, STREAMS, stream, head_width), LOW),
        qry=vmem((lines, STREAMS, stream, head_width), LOW),
        gmix=vmem((STREAMS, stream, head_width), LOW),
        dqkv=vmem((lines, 3, STREAMS, stream, head_width), LOW),
        kv=vmem((lines, 2, total, head_width), LOW),
        soft=vmem((lines, heads, local, total), F32),
        dkv_all=vmem((2, total, head_width), F32),
        dkv_out=vmem((lines, 2, local, head_width), LOW),
        dkv_in=vmem((lines, 2, local, head_width), LOW),
        part=vmem((4, STREAMS, stream, width), LOW),
        arrived=vmem((lines, 4, STREAMS, peers, sub, width), LOW),
        out_low=vmem((lines, rows, width), LOW),
        grad_low=vmem((lines, rows, width), LOW),
        norm_part=vmem((lines, 8, width), F32),
        norm_all=vmem((lines, 8, width), F32),
        w_first_s=dma((4, 2)),
        w_first_r=dma((lines, 4)),
        w_second_s=dma((lines, 4)),
        w_second_r=dma((lines, 4, 2)),
        w_core_s=dma((lines, 4)),
        w_core_r=dma((lines, 4)),
        w_own=dma((4,)),
        small_s=dma((lines - 1,)),
        small_r=dma((lines,)),
        count_s=dma((lines - 1,)),
        count_r=dma((lines,)),
        ag_s=dma((4, STREAMS, peers)),
        ag_r=dma((4, STREAMS, peers)),
        rs_s=dma((4, STREAMS, peers)),
        rs_r=dma((4, STREAMS, peers)),
        kv_s=dma((lines,)),
        kv_r=dma((lines,)),
        dkv_s=dma((lines,)),
        dkv_r=dma((lines,)),
        rows_s=dma((8, lines, 2)),
        rows_r=dma((8,)),
        share_s=dma((4,)),
        share_r=dma((4,)),
        out_s=dma((lines,)),
        out_r=dma,
        grad_s=dma((lines,)),
        grad_r=dma,
        norm_s=dma((lines,)),
        norm_r=dma,
        ends_s=dma((2 * chips - 1,)),
        ends_r=dma,
    )
    names = tuple(operands) + tuple(outputs) + tuple(scratch)
    results = pl.pallas_call(
        functools.partial(relay_kernel, names),
        out_shape=[jax.ShapeDtypeStruct(shape, kind) for shape, kind in outputs.values()],
        in_specs=[pl.BlockSpec(memory_space=space(name)) for name in operands],
        out_specs=[
            pl.BlockSpec(memory_space=pl.ANY if name in gathered else pltpu.VMEM)
            for name in outputs
        ],
        scratch_shapes=list(scratch.values()),
        compiler_params=pltpu.CompilerParams(
            collective_id=0, has_side_effects=True, vmem_limit_bytes=60 * 2**20
        ),
        name="relay",
    )(*operands.values())
    return dict(zip(outputs, results))


def weights_kernel(names, *refs):
    r = types.SimpleNamespace(**dict(zip(names, refs)))
    step = pl.program_id(0)
    micro_count, rows, buckets, width = r.activations.shape
    chips, units, head_width = r.ends.shape[0] // 2, r.all_act.shape[-1], r.all_mix.shape[-1]

    @pl.when(step == 0)
    def _():
        sums = r.ends[0]
        for other in range(1, 2 * chips):
            sums = sums + r.ends[other]
        singles = (r.ln1_gain, r.ln1_shift, r.ln2_gain, r.ln2_shift, r.b_out, r.b_proj)
        for place, single in enumerate(singles):
            single[...] = sums[place : place + 1]
        for chip in range(chips):
            both = r.ends[chip] + r.ends[chips + chip]
            r.b_fc[:, chip * units : (chip + 1) * units] = both[6:7, :units]
            here = slice(chip * head_width, (chip + 1) * head_width)
            r.b_qv[0:1, here] = both[7:8, :head_width]
            r.b_qv[1:2, here] = both[7:8, width // 2 : width // 2 + head_width]
        for target, source in ((r.activations, r.acts), (r.in_grads, r.grads)):
            for micro in range(micro_count):
                rows_of = [
                    source[micro * buckets + bucket].astype(F32)[:, None, :]
                    for bucket in range(buckets)
                ]
                target[micro] = jnp.concatenate(rows_of, axis=1).astype(LOW)
        for target in (r.w_qkv, r.w_out, r.w_fc, r.w_proj):
            target[...] = jnp.zeros_like(target)

    def rows_of_sequence(ref):
        return ref[0].reshape(2 * chips * rows, ref.shape[-1])

    nrm, nmlp, ups, brn, act, gpre, mix = (
        rows_of_sequence(ref)
        for ref in (r.all_nrm, r.all_nmlp, r.all_ups, r.all_brn, r.all_act, r.all_gpre, r.all_mix)
    )
    r.w_proj[...] += dot_tn(act, ups)
    r.w_fc[...] += dot_tn(nmlp, gpre)
    r.w_out[...] += dot_tn(mix, brn)
    for which in range(3):
        grad = r.all_dqkv[0, :, which].reshape(2 * chips * rows, head_width)
        r.w_qkv[which] += dot_tn(grad, nrm)


def weights_call(relayed, inputs_shape, head_width, units):
    lines = lax.axis_size("section")
    chips = lax.axis_size("tensor")
    width = inputs_shape[-1]
    half = width // 2
    outputs = dict(
        activations=(inputs_shape, LOW),
        in_grads=(inputs_shape, LOW),
        ln1_gain=((1, width), F32),
        ln1_shift=((1, width), F32),
        w_qkv=((3, head_width, half), F32),
        b_qv=((2, width), F32),
        w_out=((head_width, half), F32),
        b_out=((1, width), F32),
        ln2_gain=((1, width), F32),
        ln2_shift=((1, width), F32),
        w_fc=((half, units), F32),
        b_fc=((1, chips * units), F32),
        w_proj=((units, half), F32),
        b_proj=((1, width), F32),
    )

    def spec(array):
        if len(array.shape) < 5:
            return pl.BlockSpec(array.shape, lambda step: (0,) * len(array.shape))
        return pl.BlockSpec(
            (1,) + array.shape[1:], lambda step: (step,) + (0,) * (len(array.shape) - 1)
        )

    def whole(shape):
        return pl.BlockSpec(shape, lambda step: (0,) * len(shape))

    return pl.pallas_call(
        functools.partial(weights_kernel, tuple(relayed) + tuple(outputs)),
        out_shape=[jax.ShapeDtypeStruct(shape, kind) for shape, kind in outputs.values()],
        grid=(lines,),
        in_specs=[spec(array) for array in relayed.values()],
        out_specs=[whole(shape) for shape, _ in outputs.values()],
        compiler_params=pltpu.CompilerParams(vmem_limit_bytes=60 * 2**20),
        name="weight_gradients",
    )(*relayed.values())


def on_line(
    inputs,
    cotangent,
    lengths,
    chosen,
    ln1_gain,
    ln1_shift,
    w_qkv,
    b_qv,
    w_out,
    b_out,
    ln2_gain,
    ln2_shift,
    w_fc,
    b_fc,
    w_proj,
    b_proj,
):
    head_width, units = w_out.shape[1], w_fc.shape[2]
    singles = dict(
        ln1_gain=ln1_gain,
        ln1_shift=ln1_shift,
        ln2_gain=ln2_gain,
        ln2_shift=ln2_shift,
        b_out=b_out,
        b_proj=b_proj,
        b_fc=b_fc,
        b_qv=b_qv[0],
    )
    weights = dict(
        wq_in=jnp.swapaxes(w_qkv[0], 1, 2).reshape(-1, inputs.shape[-1]),
        wo_in=w_out[0],
        wf_in=w_fc[0],
        wp_in=w_proj[0],
    )
    picks = chosen.reshape((-1,) + chosen.shape[-2:])
    relayed = relay_call(inputs, cotangent, lengths, picks, singles, weights)
    results = list(weights_call(relayed, inputs.shape, head_width, units))
    results[4] = jnp.swapaxes(results[4], 1, 2)
    vectors = (2, 3, 7, 8, 9, 11, 13)
    return tuple(
        result if place in vectors else result[None] for place, result in enumerate(results)
    )


def fits_lines(mesh):
    return mesh.shape["section"] == 4 and mesh.shape["seq"] == 2 and mesh.shape["tensor"] == 4


def solution(mesh):
    placed = (
        P(None, ("seq", "tensor"), None, None),
        P(None, ("seq", "tensor"), None, None),
        P(),
        P("section", None, None, "tensor", "seq", None),
        P("section", None),
        P("section", None),
        P("section", None, None, "tensor"),
        P("section", None, "tensor"),
        P("section", "tensor", None),
        P("section", None),
        P("section", None),
        P("section", None),
        P("section", None, "tensor"),
        P("section", "tensor"),
        P("section", "tensor", None),
        P("section", None),
    )
    return jax.shard_map(
        on_line if fits_lines(mesh) else on_device,
        mesh=mesh,
        in_specs=placed,
        out_specs=(
            P("section", None, ("seq", "tensor"), None, None),
            P("section", None, ("seq", "tensor"), None, None),
            P("section", None),
            P("section", None),
            P("section", None, "seq", "tensor"),
            P("section", None, None),
            P("section", "tensor", "seq"),
            P("section", None),
            P("section", None),
            P("section", None),
            P("section", "seq", "tensor"),
            P("section", None),
            P("section", "tensor", "seq"),
            P("section", None),
        ),
        check_vma=False,
    )
```

```python
import functools
import types

import jax
import jax.numpy as jnp
from jax import lax
from jax.experimental import pallas as pl
from jax.experimental.pallas import tpu as pltpu
from jax.sharding import PartitionSpec as P

HDIM = 64
WIN = 64
QB = 64
KSEL = 64


NORM_EPS = 1e-05
MASKED = -1000000000.0


def from_behind(value, axis, steps):
    count = lax.axis_size(axis)
    first, last = (max(0, -steps), min(count, count - steps))
    return lax.ppermute(value, axis, [(source, source + steps) for source in range(first, last)])


def layer_norm(values, gain, shift):
    average = jnp.mean(values, axis=-1, keepdims=True)
    centred = values - average
    variance = jnp.mean(centred * centred, axis=-1, keepdims=True)
    return centred * lax.rsqrt(variance + NORM_EPS) * gain + shift


def gelu_tanh(values):
    return (
        0.5
        * values
        * (1.0 + jnp.tanh(0.7978845608028654 * (values + 0.044715 * values * values * values)))
    )


def gather_rows(row_block):
    return lax.all_gather(row_block, "tensor", axis=0, tiled=True)


def scatter_product(left_rows, weight, formula):
    return lax.psum_scatter(
        jnp.einsum(formula, left_rows, weight, preferred_element_type=jnp.float32).astype(
            jnp.bfloat16
        ),
        "tensor",
        scatter_dimension=0,
        tiled=True,
    ).astype(jnp.float32)


def near_slabs(full_rows, seq_start, seq_first, length_local):
    buckets = full_rows.shape[1]
    heads_local = full_rows.shape[2] // HDIM
    blocks = length_local // QB
    earlier = lax.dynamic_slice_in_dim(full_rows, jnp.maximum(seq_start - WIN, 0), WIN, 0)
    earlier = jnp.where(seq_first, jnp.zeros_like(earlier), earlier)
    local_part = lax.dynamic_slice_in_dim(full_rows, seq_start, length_local, 0)
    segment = jnp.concatenate([earlier, local_part], 0).reshape(
        length_local + WIN, buckets, heads_local, HDIM
    )
    return jnp.concatenate(
        [
            segment[offset_index * QB : offset_index * QB + length_local].reshape(
                blocks, QB, buckets, heads_local, HDIM
            )
            for offset_index in range(WIN // QB + 1)
        ],
        1,
    )


def far_rows(full_rows, flat_index):
    total_rows, buckets, feature_width = full_rows.shape
    heads_local = feature_width // HDIM
    return jnp.take(full_rows.reshape(total_rows * buckets * heads_local, HDIM), flat_index, axis=0)


def key_geometry(chosen_now, seq_start, blocks):
    buckets, heads_local = (chosen_now.shape[0], chosen_now.shape[1])
    bucket_ids = lax.broadcasted_iota(jnp.int32, chosen_now.shape, 0)
    head_ids = lax.broadcasted_iota(jnp.int32, chosen_now.shape, 1)
    flat_index = (chosen_now * buckets + bucket_ids) * heads_local + head_ids
    block_start = seq_start + QB * lax.broadcasted_iota(jnp.int32, (blocks, 1, 1), 0)
    query_ids = lax.broadcasted_iota(jnp.int32, (1, QB, 1), 1)
    key_ids = lax.broadcasted_iota(jnp.int32, (1, 1, WIN + QB), 2)
    distance = query_ids + WIN - key_ids
    near_ok = (distance >= 0) & (distance < WIN) & (block_start + key_ids - WIN >= 0)
    far_ok = chosen_now + WIN <= block_start.reshape(1, 1, blocks, 1)
    near_mask = jnp.broadcast_to(
        near_ok[:, None, None], (blocks, buckets, heads_local, QB, WIN + QB)
    )
    far_mask = jnp.broadcast_to(
        jnp.transpose(far_ok, (2, 0, 1, 3))[:, :, :, None, :],
        (blocks, buckets, heads_local, QB, KSEL),
    )
    return (flat_index, jnp.concatenate([near_mask, far_mask], -1))


def attention_setup(queries, key_rows, value_rows, chosen_now, seq_start, seq_first):
    length_local, buckets, feature_width = queries.shape
    heads_local = feature_width // HDIM
    blocks = length_local // QB
    query_blocks = queries.reshape(blocks, QB, buckets, heads_local, HDIM)
    flat_index, key_mask = key_geometry(chosen_now, seq_start, blocks)
    near_keys = near_slabs(key_rows, seq_start, seq_first, length_local)
    near_values = near_slabs(value_rows, seq_start, seq_first, length_local)
    far_keys = far_rows(key_rows, flat_index)
    far_values = far_rows(value_rows, flat_index)
    near_scores = jnp.einsum(
        "bqnhe,btnhe->bnhqt", query_blocks, near_keys, preferred_element_type=jnp.float32
    )
    far_scores = jnp.einsum(
        "bqnhe,nhbke->bnhqk", query_blocks, far_keys, preferred_element_type=jnp.float32
    )
    scores = jnp.where(
        key_mask, HDIM ** (-0.5) * jnp.concatenate([near_scores, far_scores], -1), MASKED
    )
    return (query_blocks, near_keys, near_values, far_keys, far_values, flat_index, scores)


def attend(queries, key_rows, value_rows, chosen_now, seq_start, seq_first):
    query_blocks, near_keys, near_values, far_keys, far_values, flat_index, scores = (
        attention_setup(queries, key_rows, value_rows, chosen_now, seq_start, seq_first)
    )
    span = WIN + QB
    row_top = jnp.max(scores, -1, keepdims=True)
    exp_terms = jnp.exp(scores - row_top)
    row_total = jnp.sum(exp_terms, -1, keepdims=True)
    softmax_low = (exp_terms / row_total).astype(jnp.bfloat16)
    near_part = jnp.einsum(
        "bnhqt,btnhe->bqnhe",
        softmax_low[..., :span],
        near_values,
        preferred_element_type=jnp.float32,
    )
    far_part = jnp.einsum(
        "bnhqk,nhbke->bqnhe",
        softmax_low[..., span:],
        far_values,
        preferred_element_type=jnp.float32,
    )
    return ((near_part + far_part).reshape(queries.shape), row_top + jnp.log(row_total))


def spread_back(near_grad, far_grad, flat_index, seq_start, seq_first, total_rows):
    blocks, span, buckets, heads_local, head_size = near_grad.shape
    length_local = blocks * QB
    feature_width = heads_local * head_size
    segment = jnp.zeros((length_local + WIN, buckets, heads_local, head_size), jnp.float32)
    for offset_index in range(WIN // QB + 1):
        piece = near_grad[:, offset_index * QB : (offset_index + 1) * QB].reshape(
            length_local, buckets, heads_local, head_size
        )
        segment = segment.at[offset_index * QB : offset_index * QB + length_local].add(piece)
    full_rows = jnp.zeros((total_rows * buckets * heads_local, head_size), jnp.float32)
    full_rows = full_rows.at[flat_index.reshape(-1)].add(far_grad.reshape(-1, head_size))
    full_rows = full_rows.reshape(total_rows, buckets, feature_width)
    local_part = segment[WIN:].reshape(length_local, buckets, feature_width)
    earlier = jnp.where(seq_first, 0.0, segment[:WIN].reshape(WIN, buckets, feature_width))
    full_rows = lax.dynamic_update_slice_in_dim(
        full_rows,
        lax.dynamic_slice_in_dim(full_rows, seq_start, length_local, 0) + local_part,
        seq_start,
        0,
    )
    earlier_start = jnp.maximum(seq_start - WIN, 0)
    full_rows = lax.dynamic_update_slice_in_dim(
        full_rows,
        lax.dynamic_slice_in_dim(full_rows, earlier_start, WIN, 0) + earlier,
        earlier_start,
        0,
    )
    return full_rows


def attend_back(
    queries, key_rows, value_rows, chosen_now, seq_start, seq_first, log_total, grad_mixed
):
    query_blocks, near_keys, near_values, far_keys, far_values, flat_index, scores = (
        attention_setup(queries, key_rows, value_rows, chosen_now, seq_start, seq_first)
    )
    span = WIN + QB
    score_scale = HDIM ** (-0.5)
    grad_blocks = grad_mixed.reshape(query_blocks.shape)
    weights_full = jnp.exp(scores - log_total)
    softmax_low = weights_full.astype(jnp.bfloat16)
    grad_near_weights = jnp.einsum(
        "bqnhe,btnhe->bnhqt", grad_blocks, near_values, preferred_element_type=jnp.float32
    )
    grad_far_weights = jnp.einsum(
        "bqnhe,nhbke->bnhqk", grad_blocks, far_values, preferred_element_type=jnp.float32
    )
    grad_weights = jnp.concatenate([grad_near_weights, grad_far_weights], -1)
    row_dot = jnp.sum(weights_full * grad_weights, -1, keepdims=True)
    grad_scores = (weights_full * (grad_weights - row_dot)).astype(jnp.bfloat16)
    grad_near, grad_far = (grad_scores[..., :span], grad_scores[..., span:])
    grad_queries = score_scale * (
        jnp.einsum("bnhqt,btnhe->bqnhe", grad_near, near_keys, preferred_element_type=jnp.float32)
        + jnp.einsum("bnhqk,nhbke->bqnhe", grad_far, far_keys, preferred_element_type=jnp.float32)
    )
    near_key_grad = score_scale * jnp.einsum(
        "bnhqt,bqnhe->btnhe", grad_near, query_blocks, preferred_element_type=jnp.float32
    )
    far_key_grad = score_scale * jnp.einsum(
        "bnhqk,bqnhe->nhbke", grad_far, query_blocks, preferred_element_type=jnp.float32
    )
    near_value_grad = jnp.einsum(
        "bnhqt,bqnhe->btnhe",
        softmax_low[..., :span],
        grad_blocks,
        preferred_element_type=jnp.float32,
    )
    far_value_grad = jnp.einsum(
        "bnhqk,bqnhe->nhbke",
        softmax_low[..., span:],
        grad_blocks,
        preferred_element_type=jnp.float32,
    )
    total_rows = key_rows.shape[0]
    key_grad = spread_back(
        near_key_grad, far_key_grad, flat_index, seq_start, seq_first, total_rows
    )
    value_grad = spread_back(
        near_value_grad, far_value_grad, flat_index, seq_start, seq_first, total_rows
    )
    return (grad_queries.reshape(queries.shape), key_grad, value_grad)


def forward_pass(hidden, params, chosen_now, query_mask, seq_start, seq_first, finish):
    (
        ln1_gain,
        ln1_shift,
        w_qkv,
        b_qv,
        w_out,
        b_out,
        ln2_gain,
        ln2_shift,
        w_fc,
        b_fc,
        w_proj,
        b_proj,
    ) = params
    hidden_wide = hidden.astype(jnp.float32)
    normed_all = gather_rows(layer_norm(hidden_wide, ln1_gain, ln1_shift).astype(jnp.bfloat16))
    projected = jnp.einsum("pnd,jdc->jpnc", normed_all, w_qkv, preferred_element_type=jnp.float32)
    queries = (projected[0] + b_qv[0]).astype(jnp.bfloat16)
    key_rows, value_rows = (
        lax.all_gather(projected[1].astype(jnp.bfloat16), "seq", axis=0, tiled=True),
        lax.all_gather((projected[2] + b_qv[1]).astype(jnp.bfloat16), "seq", axis=0, tiled=True),
    )
    attended, log_total = attend(queries, key_rows, value_rows, chosen_now, seq_start, seq_first)
    mixed_rows = (attended * query_mask[:, :, None]).astype(jnp.bfloat16)
    middle = hidden_wide + scatter_product(mixed_rows, w_out, "pnc,cd->pnd") + b_out
    normed_mlp = gather_rows(layer_norm(middle, ln2_gain, ln2_shift).astype(jnp.bfloat16))
    pre_active = (
        jnp.einsum("pnd,df->pnf", normed_mlp, w_fc, preferred_element_type=jnp.float32) + b_fc
    )
    active = gelu_tanh(pre_active).astype(jnp.bfloat16)
    if not finish:
        return (
            normed_all,
            queries,
            key_rows,
            value_rows,
            log_total,
            mixed_rows,
            middle,
            normed_mlp,
            pre_active,
            active,
        )
    output = (middle + scatter_product(active, w_proj, "pnf,fd->pnd") + b_proj).astype(jnp.bfloat16)
    return (output, (key_rows, value_rows))


def backward_pass(hidden, upstream, params, chosen_now, query_mask, seq_start, seq_first):
    (
        ln1_gain,
        ln1_shift,
        w_qkv,
        b_qv,
        w_out,
        b_out,
        ln2_gain,
        ln2_shift,
        w_fc,
        b_fc,
        w_proj,
        b_proj,
    ) = params
    (
        normed_all,
        queries,
        key_rows,
        value_rows,
        log_total,
        mixed_rows,
        middle,
        normed_mlp,
        pre_active,
        active,
    ) = forward_pass(hidden, params, chosen_now, query_mask, seq_start, seq_first, False)
    upstream_all = gather_rows(upstream)
    grad_w_proj = jnp.einsum(
        "pnf,pnd->fd", active, upstream_all, preferred_element_type=jnp.float32
    )
    grad_b_proj = jnp.sum(upstream.astype(jnp.float32), axis=(0, 1))
    grad_active = jnp.einsum(
        "pnd,fd->pnf", upstream_all, w_proj, preferred_element_type=jnp.float32
    )
    unused_value, gelu_pull = jax.vjp(gelu_tanh, pre_active)
    grad_pre = gelu_pull(grad_active)[0].astype(jnp.bfloat16)
    grad_w_fc = jnp.einsum("pnd,pnf->df", normed_mlp, grad_pre, preferred_element_type=jnp.float32)
    grad_b_fc = jnp.sum(grad_pre.astype(jnp.float32), axis=(0, 1))
    grad_normed_mlp = scatter_product(grad_pre, w_fc, "pnf,df->pnd")
    unused_norm, second_pull = jax.vjp(layer_norm, middle, ln2_gain, ln2_shift)
    grad_mid_norm, grad_ln2_gain, grad_ln2_shift = second_pull(grad_normed_mlp)
    grad_middle = upstream.astype(jnp.float32) + grad_mid_norm
    grad_branch = grad_middle.astype(jnp.bfloat16)
    grad_b_out = jnp.sum(grad_branch.astype(jnp.float32), axis=(0, 1))
    branch_all = gather_rows(grad_branch)
    grad_w_out = jnp.einsum(
        "pnc,pnd->cd", mixed_rows, branch_all, preferred_element_type=jnp.float32
    )
    grad_mixed = jnp.einsum(
        "pnd,cd->pnc", branch_all, w_out, preferred_element_type=jnp.float32
    ).astype(jnp.bfloat16) * query_mask[:, :, None].astype(jnp.bfloat16)
    grad_queries, key_grad_all, value_grad_all = attend_back(
        queries, key_rows, value_rows, chosen_now, seq_start, seq_first, log_total, grad_mixed
    )
    key_grad, value_grad = (
        lax.psum_scatter(
            key_grad_all.astype(jnp.bfloat16), "seq", scatter_dimension=0, tiled=True
        ).astype(jnp.float32),
        lax.psum_scatter(
            value_grad_all.astype(jnp.bfloat16), "seq", scatter_dimension=0, tiled=True
        ).astype(jnp.float32),
    )
    grad_project = jnp.stack(
        [
            grad_queries.astype(jnp.bfloat16),
            key_grad.astype(jnp.bfloat16),
            value_grad.astype(jnp.bfloat16),
        ],
        2,
    )
    grad_w_qkv = jnp.einsum(
        "pnd,pnjc->jdc", normed_all, grad_project, preferred_element_type=jnp.float32
    )
    grad_b_qv = jnp.sum(grad_project[:, :, 0::2].astype(jnp.float32), axis=(0, 1))
    grad_normed = scatter_product(grad_project, w_qkv, "pnjc,jdc->pnd")
    unused_first, first_pull = jax.vjp(layer_norm, hidden.astype(jnp.float32), ln1_gain, ln1_shift)
    grad_in_norm, grad_ln1_gain, grad_ln1_shift = first_pull(grad_normed)
    grad_hidden = (grad_middle + grad_in_norm).astype(jnp.bfloat16)
    block_grads = (
        grad_ln1_gain,
        grad_ln1_shift,
        grad_w_qkv,
        grad_b_qv,
        grad_w_out,
        grad_b_out,
        grad_ln2_gain,
        grad_ln2_shift,
        grad_w_fc,
        grad_b_fc,
        grad_w_proj,
        grad_b_proj,
    )
    return (grad_hidden, block_grads)


def on_device(
    inputs,
    cotangent,
    lengths,
    chosen,
    ln1_gain,
    ln1_shift,
    w_qkv,
    b_qv,
    w_out,
    b_out,
    ln2_gain,
    ln2_shift,
    w_fc,
    b_fc,
    w_proj,
    b_proj,
):
    params = tuple(
        (
            weight_array[0]
            for weight_array in (
                ln1_gain,
                ln1_shift,
                w_qkv,
                b_qv,
                w_out,
                b_out,
                ln2_gain,
                ln2_shift,
                w_fc,
                b_fc,
                w_proj,
                b_proj,
            )
        )
    )
    section_index = lax.axis_index("section")
    section_count = lax.axis_size("section")
    seq_index = lax.axis_index("seq")
    tensor_index = lax.axis_index("tensor")
    tensor_count = lax.axis_size("tensor")
    micro_count, rows_local, buckets, feature_width = inputs.shape
    length_local = rows_local * tensor_count
    heads_width = w_qkv.shape[-1]
    seq_start = seq_index * length_local
    seq_first = seq_index == 0
    positions = seq_start + lax.broadcasted_iota(jnp.int32, (micro_count, length_local, buckets), 1)
    mask_all = (positions < lengths[:, None, :]).astype(jnp.float32)
    mask_rows = lax.dynamic_slice_in_dim(mask_all, tensor_index * rows_local, rows_local, 1)
    step_count = micro_count + section_count - 1
    chosen_section = chosen[0]
    received = jnp.zeros((rows_local, buckets, feature_width), jnp.bfloat16)
    stored = jnp.zeros((micro_count, rows_local, buckets, feature_width), jnp.bfloat16)
    outputs = jnp.zeros_like(stored)
    for step_index in range(step_count):
        micro_index = step_index - section_index
        running = (micro_index >= 0) & (micro_index < micro_count)
        slot_index = jnp.clip(micro_index, 0, micro_count - 1)
        block_in = jnp.where(
            section_index == 0, lax.dynamic_index_in_dim(inputs, slot_index, 0, False), received
        )
        chosen_now = lax.dynamic_index_in_dim(chosen_section, slot_index, 0, False)
        query_mask = lax.dynamic_index_in_dim(mask_all, slot_index, 0, False)
        result, key_pair = forward_pass(
            block_in, params, chosen_now, query_mask, seq_start, seq_first, True
        )
        stored = jnp.where(
            running, lax.dynamic_update_index_in_dim(stored, block_in, slot_index, 0), stored
        )
        outputs = jnp.where(
            running, lax.dynamic_update_index_in_dim(outputs, result, slot_index, 0), outputs
        )
        received = from_behind(result, "section", 1)
    back_received = jnp.zeros((rows_local, buckets, feature_width), jnp.bfloat16)
    in_grads = jnp.zeros_like(stored)
    totals = None
    for step_index in range(step_count):
        micro_index = step_index - (section_count - 1 - section_index)
        running = (micro_index >= 0) & (micro_index < micro_count)
        slot_index = jnp.clip(micro_index, 0, micro_count - 1)
        chosen_now = lax.dynamic_index_in_dim(chosen_section, slot_index, 0, False)
        query_mask = lax.dynamic_index_in_dim(mask_all, slot_index, 0, False)
        local_mask = lax.dynamic_index_in_dim(mask_rows, slot_index, 0, False)
        top_grad = (
            lax.dynamic_index_in_dim(cotangent, slot_index, 0, False).astype(jnp.float32)
            * local_mask[:, :, None]
        ).astype(jnp.bfloat16)
        upstream = jnp.where(section_index == section_count - 1, top_grad, back_received)
        hidden = lax.dynamic_index_in_dim(stored, slot_index, 0, False)
        grad_hidden, block_grads = backward_pass(
            hidden, upstream, params, chosen_now, query_mask, seq_start, seq_first
        )
        block_grads = tuple(
            (jnp.where(running, grad_part, jnp.zeros_like(grad_part)) for grad_part in block_grads)
        )
        totals = (
            block_grads
            if step_index == 0
            else tuple(
                (total_part + grad_part for total_part, grad_part in zip(totals, block_grads))
            )
        )
        in_grads = jnp.where(
            running, lax.dynamic_update_index_in_dim(in_grads, grad_hidden, slot_index, 0), in_grads
        )
        back_received = from_behind(grad_hidden, "section", -1)
    (
        sum_ln1_gain,
        sum_ln1_shift,
        sum_w_qkv,
        sum_b_qv,
        sum_w_out,
        sum_b_out,
        sum_ln2_gain,
        sum_ln2_shift,
        sum_w_fc,
        sum_b_fc,
        sum_w_proj,
        sum_b_proj,
    ) = totals
    part_qkv, part_out, part_fc, part_proj = (
        lax.psum_scatter(
            sum_w_qkv.astype(jnp.bfloat16), "seq", scatter_dimension=1, tiled=True
        ).astype(jnp.float32),
        lax.psum_scatter(
            sum_w_out.astype(jnp.bfloat16), "seq", scatter_dimension=1, tiled=True
        ).astype(jnp.float32),
        lax.psum_scatter(
            sum_w_fc.astype(jnp.bfloat16), "seq", scatter_dimension=0, tiled=True
        ).astype(jnp.float32),
        lax.psum_scatter(
            sum_w_proj.astype(jnp.bfloat16), "seq", scatter_dimension=1, tiled=True
        ).astype(jnp.float32),
    )
    bias_qv = lax.dynamic_update_slice_in_dim(
        jnp.zeros((2, feature_width), jnp.float32), sum_b_qv, tensor_index * heads_width, 1
    )
    units_local = sum_b_fc.shape[0]
    bias_fc = lax.dynamic_update_slice_in_dim(
        jnp.zeros((units_local * tensor_count,), jnp.float32),
        sum_b_fc,
        tensor_index * units_local,
        0,
    )
    small_sums = lax.psum(
        (
            sum_ln1_gain,
            sum_ln1_shift,
            bias_qv,
            sum_b_out,
            sum_ln2_gain,
            sum_ln2_shift,
            bias_fc,
            sum_b_proj,
        ),
        ("seq", "tensor"),
    )
    return (
        outputs[None],
        in_grads[None],
        small_sums[0][None],
        small_sums[1][None],
        part_qkv[None],
        small_sums[2][None],
        part_out[None],
        small_sums[3][None],
        small_sums[4][None],
        small_sums[5][None],
        part_fc[None],
        small_sums[6][None],
        part_proj[None],
        small_sums[7][None],
    )


STREAMS = 2
NRM, NMLP, UPS, BRN, ACT, GPRE, MIX, DQKV = range(8)
F32 = jnp.float32
LOW = jnp.bfloat16
MESH_ID = pl.DeviceIdType.MESH


def dot_nn(left, right):
    return lax.dot_general(left, right, (((1,), (0,)), ((), ())), preferred_element_type=F32)


def dot_nt(left, right):
    return lax.dot_general(left, right, (((1,), (1,)), ((), ())), preferred_element_type=F32)


def dot_tn(left, right):
    return lax.dot_general(left, right, (((0,), (0,)), ((), ())), preferred_element_type=F32)


def standard(rows):
    centred = rows - jnp.mean(rows, axis=-1, keepdims=True)
    scale = lax.rsqrt(jnp.mean(centred * centred, axis=-1, keepdims=True) + NORM_EPS)
    return centred * scale, scale


def standard_back(grad, xhat, scale):
    inner = jnp.mean(grad * xhat, axis=-1, keepdims=True)
    return scale * (grad - jnp.mean(grad, axis=-1, keepdims=True) - xhat * inner)


def column_sum(rows):
    return jnp.sum(rows.astype(F32), axis=0, keepdims=True)


def relay_kernel(names, *refs):
    r = types.SimpleNamespace(**dict(zip(names, refs)))
    a, c, t = (lax.axis_index(name) for name in ("section", "seq", "tensor"))
    lines = lax.axis_size("section")
    chips = lax.axis_size("tensor")
    rows, buckets, width = r.inputs.shape[1:]
    half_width = width // 2
    local = rows * chips
    total = 2 * local
    sub = rows // STREAMS
    stream_rows = local // STREAMS
    head_width = r.wo_in.shape[0]
    heads = head_width // HDIM
    blocks = local // QB
    units = r.wp_in.shape[0]
    scale = HDIM ** (-0.5)
    streams = range(STREAMS)

    def remote(src, dst, send, recv, **target):
        return pltpu.make_async_remote_copy(
            src_ref=src,
            dst_ref=dst,
            send_sem=send,
            recv_sem=recv,
            device_id=target,
            device_id_type=MESH_ID,
        )

    def drain(ref, sem):
        pltpu.make_async_copy(ref, ref, sem).wait()

    def row_block(index, size):
        return pl.ds(pl.multiple_of(index * size, size), size)

    near_chip = t + 1 - 2 * (t % 2)
    over_chip = (t + 2) % 4
    across_chip = 3 - t
    middle_chip = (t == 1) | (t == 2)
    end_chip = (t == 0) | (t == 3)
    owned = 2 * sub
    mine = row_block(t - 1, owned)
    my_half = row_block(c, local)

    barrier = pltpu.get_barrier_semaphore()
    for core in range(2):
        for step in range(1, chips):
            there = {"tensor": (t + step) % chips, "seq": core}
            pl.semaphore_signal(barrier, inc=1, device_id=there, device_id_type=MESH_ID)
        for step in range(1, lines):
            there = {"section": (a + step) % lines, "seq": core}
            pl.semaphore_signal(barrier, inc=1, device_id=there, device_id_type=MESH_ID)
    for step in range(1, lines):
        there = {"section": (a + step) % lines, "tensor": near_chip}
        pl.semaphore_signal(barrier, inc=1, device_id=there, device_id_type=MESH_ID)
    pl.semaphore_signal(barrier, inc=1, device_id={"seq": 1 - c}, device_id_type=MESH_ID)
    pl.semaphore_wait(barrier, 2 * (chips - 1) + 3 * (lines - 1) + 1)

    def beside(s):
        return s + 1 - 2 * (s % 2)

    def above(s):
        return (s + 2) % 4

    def store(p):
        return (r.wq, r.wo, r.wf, r.wp)[p]

    def source(p):
        return (r.wq_in, r.wo_in, r.wf_in, r.wp_in)[p]

    def height(p):
        return source(p).shape[0]

    def core_half(p, s, core):
        return store(p).at[s, row_block(core, height(p) // 2)]

    def first_hop(p, s, neighbour, which):
        return remote(
            source(p).at[row_block(c, height(p) // 2)],
            core_half(p, s, c),
            r.w_first_s.at[p, which],
            r.w_first_r.at[s, p],
            section=neighbour,
        )

    def second_hop(p, s, which):
        view = store(p).at[s, row_block(2 * c + which, height(p) // 4)]
        return remote(
            view, view, r.w_second_s.at[s, p], r.w_second_r.at[s, p, which], section=3 - s
        )

    def core_hop(p, s, core):
        view = core_half(p, s, core)
        return remote(view, view, r.w_core_s.at[s, p], r.w_core_r.at[s, p], seq=1 - c)

    def own_copy(p):
        return pltpu.make_async_copy(source(p), store(p).at[a], r.w_own.at[p])

    def pass_on(s, p, which):
        line = (beside(s), above(s))[which]

        @pl.when(a == line)
        def _():
            first_hop(p, s, line, which).wait_recv()
            second_hop(p, s, which).start()
            core_hop(p, s, c).start()

    def pass_later(pieces, at_first):
        for later in range(1, lines):
            for which in range(2):
                if ((beside(later), above(later))[which] == 0) == at_first:
                    for p in pieces:
                        pass_on(later, p, which)

    def pass_far(s, p):
        @pl.when(a == 3 - s)
        def _():
            second_hop(p, s, 0).wait_recv()
            second_hop(p, s, 1).wait_recv()
            core_hop(p, s, c).start()

    def need(s, p):
        @pl.when(s == 0)
        def _():
            pass_on(0, p, 0)
            pass_on(0, p, 1)
            pass_far(0, p)

        @pl.when(a == s)
        def _():
            own_copy(p).wait()

        @pl.when(a != s)
        def _():
            core_hop(p, s, 1 - c).wait_recv()

    def small_copy(step, line, slot):
        return remote(
            r.small_own, r.small.at[slot], r.small_s.at[step], r.small_r.at[slot], section=line
        )

    def count_copy(step, line, slot):
        return remote(
            r.count_own.at[line],
            r.count.at[slot],
            r.count_s.at[step],
            r.count_r.at[slot],
            section=line,
        )

    singles = (r.ln1_gain, r.ln1_shift, r.ln2_gain, r.ln2_shift, r.b_out, r.b_proj)
    for place, single in enumerate(singles):
        r.small_own[place : place + 1] = single[...]
    r.small_own[6:7, :units] = r.b_fc[...]
    r.small_own[7:8, :head_width] = r.b_qv[0:1]
    r.small_own[7:8, half_width : half_width + head_width] = r.b_qv[1:2]
    for step in range(1, lines):
        small_copy(step - 1, (a + step) % lines, a).start()
    for p in range(4):
        for which, line in enumerate((beside(a), above(a))):
            first_hop(p, a, line, which).start()
    for p in range(4):
        own_copy(p).start()
    r.small[a] = r.small_own[...]

    def place_of(index):
        inside = index % local
        stream, left = inside // stream_rows, inside % stream_rows
        return (index // local) * local + (left // sub) * rows + stream * sub + left % sub

    def iota(shape, dimension):
        return lax.broadcasted_iota(jnp.int32, shape, dimension)

    square = jnp.where(iota((KSEL, KSEL), 0) == iota((KSEL, KSEL), 1), 1.0, 0.0).astype(LOW)
    position = place_of(iota((KSEL, total), 1)).astype(F32)
    for pair in range(lines * heads):
        line, head = pair // heads, pair % heads
        columns = dot_nt(square, r.chosen[pair].astype(F32).astype(LOW))
        for block in range(blocks):
            pick = head * blocks + block
            r.count_own[line, pick : pick + 1, :] = jnp.sum(
                jnp.where(columns[:, block : block + 1] == position, 1.0, 0.0),
                axis=0,
                keepdims=True,
            )
    for step in range(1, lines):
        count_copy(step - 1, (a + step) % lines, a).start()
    r.count[a] = r.count_own[a]

    NEAR, OVER, ACROSS = range(3)

    def gather(buffer, s, kind, j, owner, target, slot):
        view = buffer.at[s, j, row_block(owner - 1, owned)]
        return remote(
            view, view, r.ag_s.at[kind, j, slot], r.ag_r.at[kind, j, slot], tensor=target
        )

    def gather_start(buffer, s, kind, j):
        gather(buffer, s, kind, j, t, over_chip, OVER).start()
        gather(buffer, s, kind, j, t, across_chip, ACROSS).start()
        gather(buffer, s, kind, j, t, near_chip, NEAR).start()

    def gather_wait(buffer, s, kind, j):
        @pl.when(middle_chip)
        def _():
            gather(buffer, s, kind, j, across_chip, across_chip, ACROSS).wait_recv()

        @pl.when(end_chip)
        def _():
            gather(buffer, s, kind, j, near_chip, near_chip, NEAR).wait_recv()
            gather(buffer, s, kind, j, over_chip, over_chip, OVER).wait_recv()

    def gather_sent(buffer, s, kind, j):
        @pl.when(middle_chip)
        def _():
            gather(buffer, s, kind, j, t, over_chip, OVER).wait_send()
            gather(buffer, s, kind, j, t, across_chip, ACROSS).wait_send()
            gather(buffer, s, kind, j, t, near_chip, NEAR).wait_send()

    def scatter(s, kind, j, owner, slot):
        return remote(
            r.part.at[kind, j, row_block(owner - 1, owned)],
            r.arrived.at[s, kind, j, slot],
            r.rs_s.at[kind, j, slot],
            r.rs_r.at[kind, j, slot],
            tensor=owner,
        )

    def scatter_start(s, kind, j, product):
        r.part[kind, j] = product.astype(LOW)

        @pl.when(end_chip)
        def _():
            scatter(s, kind, j, over_chip, OVER).start()
            scatter(s, kind, j, near_chip, NEAR).start()

        @pl.when(middle_chip)
        def _():
            scatter(s, kind, j, across_chip, ACROSS).start()

    def scatter_sum(s, kind, j):
        result = r.part[kind, j, mine].astype(F32)
        for slot in (NEAR, ACROSS, OVER):
            scatter(s, kind, j, t, slot).wait_recv()
            result = result + r.arrived[s, kind, j, slot].astype(F32)
        return result

    def scatter_sent(s, kind, j):
        @pl.when(end_chip)
        def _():
            scatter(s, kind, j, over_chip, OVER).wait_send()
            scatter(s, kind, j, near_chip, NEAR).wait_send()

        @pl.when(middle_chip)
        def _():
            scatter(s, kind, j, across_chip, ACROSS).wait_send()

    own_rows = (r.nrm, r.nmlp, r.ups, r.brn, r.act, r.gpre, r.mix, r.dqkv)
    all_rows = (
        r.all_nrm,
        r.all_nmlp,
        r.all_ups,
        r.all_brn,
        r.all_act,
        r.all_gpre,
        r.all_mix,
        r.all_dqkv,
    )

    def rows_copy(index, s, same, stays=False):
        core = c if same else 1 - c
        src = own_rows[index].at[s]
        dst = all_rows[index].at[a, c]
        if index <= BRN:
            src = src.at[:, :, row_block(core, half_width)]
        recv = r.rows_r.at[index]
        if stays:
            return pltpu.make_async_copy(src, dst, recv)
        if same:
            return remote(src, dst, r.rows_s.at[index, s, 0], recv, section=s)
        return remote(src, dst, r.rows_s.at[index, s, 1], recv, section=s, seq=1 - c)

    def rows_start(index, s):
        @pl.when(a == s)
        def _():
            rows_copy(index, s, True, True).start()

        @pl.when(a != s)
        def _():
            rows_copy(index, s, True).start()

        if index <= BRN:
            rows_copy(index, s, False).start()

    def rows_sent(index, s):
        @pl.when(a != s)
        def _():
            rows_copy(index, s, True).wait_send()

        if index <= BRN:
            rows_copy(index, s, False).wait_send()

    def share_copy(index, core):
        view = all_rows[index].at[:, core]
        return remote(view, view, r.share_s.at[index - ACT], r.share_r.at[index - ACT], seq=1 - c)

    def share(index):
        drain(all_rows[index].at[:, c], r.rows_r.at[index])
        share_copy(index, c).start()

    def norm_copy(s):
        return remote(
            r.norm_part.at[s], r.norm_all.at[a], r.norm_s.at[s], r.norm_r, section=s
        )

    def norm_start(s):
        @pl.when(a == s)
        def _():
            pltpu.make_async_copy(r.norm_part.at[s], r.norm_all.at[a], r.norm_r).start()

        @pl.when(a != s)
        def _():
            norm_copy(s).start()

    def home_copy(what, s, chip):
        src, dst, send, recv = what
        return remote(
            src.at[s, chip % 2],
            dst.at[a],
            send.at[s, chip % 2],
            recv,
            section=s,
            tensor=chip,
        )

    def home_start(what, s):
        src, dst, send, recv = what

        @pl.when(middle_chip & (a == s))
        def _():
            pltpu.make_async_copy(src.at[s, t % 2], dst.at[a], recv).start()

        @pl.when(middle_chip & (a != s))
        def _():
            home_copy(what, s, t).start()

        @pl.when(middle_chip)
        def _():
            home_copy(what, s, near_chip).start()

    def home_sent(what, s):
        @pl.when(middle_chip & (a != s))
        def _():
            home_copy(what, s, t).wait_send()

        @pl.when(middle_chip)
        def _():
            home_copy(what, s, near_chip).wait_send()

    out_home = (r.out_low, r.acts, r.out_s, r.out_r)
    grad_home = (r.grad_low, r.grads, r.grad_s, r.grad_r)

    length = r.lengths[a // buckets, a % buckets]
    query = place_of(c * local + iota((local, total), 0))
    key = place_of(iota((local, total), 1))
    near = jnp.where((query >= key) & (query - key < WIN), 1.0, 0.0)
    key_row = place_of(iota((1, total), 1))
    block_of = place_of(iota((local, total), 0)) // QB

    def row_mask(place):
        return jnp.where(place < length, 1.0, 0.0)

    def multiplicity(s, head):
        times = near
        for block in range(blocks):
            pick = head * blocks + block
            limit = (c * blocks + block) * QB - WIN
            counted = jnp.where(key_row <= limit, r.count[s, pick : pick + 1, :], 0.0)
            times = times + jnp.where(block_of == block, counted, 0.0)
        return times

    def head_cols(head):
        return slice(head * HDIM, (head + 1) * HDIM)

    def kv_copy(s, core):
        view = r.kv.at[s, :, row_block(core, local)]
        return remote(view, view, r.kv_s.at[s], r.kv_r.at[s], seq=1 - c)

    def dkv_copy(s):
        return remote(r.dkv_out.at[s], r.dkv_in.at[s], r.dkv_s.at[s], r.dkv_r.at[s], seq=1 - c)

    def flat(array):
        return array.reshape(local, array.shape[-1])

    def own_sequence(ref):
        both = ref[a // buckets].astype(F32)
        picked = both[:, 0, :]
        for bucket in range(1, buckets):
            picked = jnp.where(a % buckets == bucket, both[:, bucket, :], picked)
        return picked

    def first_copy():
        return remote(r.first_out, r.first_in, r.first_s, r.first_r, tensor=near_chip)

    own_place = c * local + t * rows + iota((rows, 1), 0)
    r.first_out[0] = own_sequence(r.inputs).astype(LOW)
    r.first_out[1] = (own_sequence(r.cotangent) * row_mask(own_place)).astype(LOW)
    r.norm_part[...] = jnp.zeros_like(r.norm_part)

    @pl.when(end_chip)
    def _():
        first_copy().start()

    @pl.when(middle_chip)
    def _():
        first_copy().wait_recv()
        for which in range(2):
            here, beside_it = r.first_out[which].astype(F32), r.first_in[which].astype(F32)
            lower = jnp.where(t % 2 == 0, here, beside_it)
            upper = jnp.where(t % 2 == 0, beside_it, here)
            for j in streams:
                part = slice(j * sub, (j + 1) * sub)
                own_block = jnp.concatenate([lower[part], upper[part]], axis=0)
                if which == 0:
                    r.hidden[j] = own_block
                else:
                    r.upstream[j] = own_block.astype(LOW)

    def on_owner(stage):
        def run(s, j):
            @pl.when(middle_chip)
            def _():
                stage(s, j)

        return run

    def keep_rows(target, s, j, result):
        for half in range(2):
            target[s, half, j * sub : (j + 1) * sub] = result[half * sub : (half + 1) * sub]

    @on_owner
    def enter(s, j):
        xhat, inverse = standard(r.hidden[j])
        r.xhat1[s, j] = xhat
        r.inv1[s, j] = jnp.broadcast_to(inverse, (owned, 128))
        r.nrm[s, j, mine] = (xhat * r.small[s, 0:1] + r.small[s, 1:2]).astype(LOW)
        gather_start(r.nrm, s, 0, j)

    def project(s, j):
        gather_wait(r.nrm, s, 0, j)
        normed = r.nrm[s, j]
        place = row_block(c * STREAMS + j, stream_rows)
        bias_v = r.small[s, 7:8, half_width : half_width + head_width]
        key_rows = dot_nt(normed, r.wq[s, head_width : 2 * head_width])
        value_rows = dot_nt(normed, r.wq[s, 2 * head_width : 3 * head_width]) + bias_v
        r.kv[s, 0, place] = key_rows.astype(LOW)
        r.kv[s, 1, place] = value_rows.astype(LOW)
        gather_sent(r.nrm, s, 0, j)

    def ask(s, j):
        queries = dot_nt(r.nrm[s, j], r.wq[s, 0:head_width]) + r.small[s, 7:8, :head_width]
        r.qry[s, j] = queries.astype(LOW)

    def attend_line(s):
        mixed = []
        queries = flat(r.qry[s])
        for head in range(heads):
            times = multiplicity(s, head)
            scores = scale * dot_nt(queries[:, head_cols(head)], r.kv[s, 0, :, head_cols(head)])
            scores = jnp.where(times > 0.0, scores, MASKED)
            top = jnp.max(scores, axis=-1, keepdims=True)
            terms = times * jnp.exp(scores - top)
            weights = terms / jnp.sum(terms, axis=-1, keepdims=True)
            r.soft[s, head] = weights
            mixed.append(dot_nn(weights.astype(LOW), r.kv[s, 1, :, head_cols(head)]))
        mask = row_mask(place_of(c * local + iota((local, 1), 0)))
        mixed = (jnp.concatenate(mixed, axis=-1) * mask).astype(LOW)
        r.mix[s] = mixed.reshape(r.mix.shape[1:])

    def leave_attention(s, j):
        scatter_start(s, 0, j, dot_nn(r.mix[s, j], r.wo[s]))

    @on_owner
    def between(s, j):
        middle = r.hidden[j] + scatter_sum(s, 0, j) + r.small[s, 4:5]
        r.middle[j] = middle
        xhat, inverse = standard(middle)
        r.xhat2[s, j] = xhat
        r.inv2[s, j] = jnp.broadcast_to(inverse, (owned, 128))
        r.nmlp[s, j, mine] = (xhat * r.small[s, 2:3] + r.small[s, 3:4]).astype(LOW)
        gather_start(r.nmlp, s, 1, j)

    def feed(s, j):
        gather_wait(r.nmlp, s, 1, j)
        before = dot_nn(r.nmlp[s, j], r.wf[s]) + r.small[s, 6:7, :units]
        bend = jnp.tanh(0.7978845608028654 * (before + 0.044715 * before * before * before))
        r.act[s, j] = (0.5 * before * (1.0 + bend)).astype(LOW)
        r.slope[s, j] = 0.5 * (1.0 + bend) + 0.5 * before * (1.0 - bend * bend) * (
            0.7978845608028654 * (1.0 + 3 * 0.044715 * before * before)
        )

        gather_sent(r.nmlp, s, 1, j)

    def leave_feed(s, j):
        scatter_start(s, 1, j, dot_nn(r.act[s, j], r.wp[s]))

    @on_owner
    def finish(s, j):
        result = r.middle[j] + scatter_sum(s, 1, j) + r.small[s, 5:6]
        keep_rows(r.out_low, s, j, result.astype(LOW))
        r.hidden[j] = result.astype(LOW).astype(F32)

    def small_ready(s):
        @pl.when(a != s)
        def _():
            small_copy(0, a, s).wait_recv()

    small_ready(0)
    for j in streams:
        enter(0, j)

    def forward(s, _):
        need(s, 0)
        for j in streams:
            project(s, j)
        kv_copy(s, c).start()
        for j in streams:
            ask(s, j)
        rows_start(NRM, s)

        @pl.when(a != s)
        def _():
            count_copy(0, a, s).wait_recv()

        kv_copy(s, 1 - c).wait_recv()
        attend_line(s)
        need(s, 1)
        for j in streams:
            leave_attention(s, j)
        rows_start(MIX, s)

        @pl.when(s == 0)
        def _():
            pass_later((0, 1), False)

        @pl.when(s > 0)
        def _():
            pass_far(s, 2)
            pass_far(s, 3)

        for j in streams:
            between(s, j)
            scatter_sent(s, 0, j)
        need(s, 2)

        @pl.when(s == 0)
        def _():
            pass_later((2,), False)

        for j in streams:
            feed(s, j)
            if j == 0:
                need(s, 3)
            leave_feed(s, j)

        @pl.when(s == 0)
        def _():
            pass_later((3,), False)

        rows_start(NMLP, s)
        rows_start(ACT, s)

        @pl.when(s + 1 < lines)
        def _():
            small_ready(s + 1)

        for j in streams:
            finish(s, j)
            scatter_sent(s, 1, j)

            @pl.when(s + 1 < lines)
            def _():
                enter(s + 1, j)

        home_start(out_home, s)

        @pl.when(s == 0)
        def _():
            pass_later(range(4), True)

        @pl.when(s + 1 < lines)
        def _():
            pass_far(s + 1, 0)
            pass_far(s + 1, 1)

        return 0

    lax.fori_loop(0, lines, forward, 0)

    @on_owner
    def turn(s, j):
        upstream = r.upstream[j]
        r.ups[s, j, mine] = upstream
        gather_start(r.ups, s, 2, j)
        r.norm_part[s, 5:6] += column_sum(upstream)

    def feed_back(s, j):
        gather_wait(r.ups, s, 2, j)
        grad_pre = (dot_nt(r.ups[s, j], r.wp[s]) * r.slope[s, j]).astype(LOW)
        r.gpre[s, j] = grad_pre
        scatter_start(s, 2, j, dot_nt(grad_pre, r.wf[s]))
        r.norm_part[s, 6:7, :units] += column_sum(grad_pre)
        gather_sent(r.ups, s, 2, j)

    @on_owner
    def between_back(s, j):
        grad = scatter_sum(s, 2, j)
        xhat = r.xhat2[s, j]
        upstream = r.upstream[j].astype(F32)
        grad_middle = upstream + standard_back(
            grad * r.small[s, 2:3], xhat, r.inv2[s, j, :, 0:1]
        )
        r.middle[j] = grad_middle
        branch = grad_middle.astype(LOW)
        r.brn[s, j, mine] = branch
        gather_start(r.brn, s, 3, j)
        r.norm_part[s, 2:3] += column_sum(grad * xhat)
        r.norm_part[s, 3:4] += column_sum(grad)
        r.norm_part[s, 4:5] += column_sum(branch)

    def mixed_back(s, j):
        gather_wait(r.brn, s, 3, j)
        place = place_of(c * local + j * stream_rows + iota((stream_rows, 1), 0))
        r.gmix[j] = (dot_nt(r.brn[s, j], r.wo[s]) * row_mask(place)).astype(LOW)
        gather_sent(r.brn, s, 3, j)

    def attend_line_back(s):
        grad_q, grad_k, grad_v = [], [], []
        grad_mixed = flat(r.gmix[...])
        queries = flat(r.qry[s])
        for head in range(heads):
            cols = head_cols(head)
            weights = r.soft[s, head]
            grad_head = grad_mixed[:, cols]
            grad_weights = dot_nt(grad_head, r.kv[s, 1, :, cols])
            inner = jnp.sum(weights * grad_weights, axis=-1, keepdims=True)
            grad_scores = (weights * (grad_weights - inner)).astype(LOW)
            grad_k.append(scale * dot_tn(grad_scores, queries[:, cols]))
            grad_v.append(dot_tn(weights.astype(LOW), grad_head))
            grad_q.append(scale * dot_nn(grad_scores, r.kv[s, 0, :, cols]))
        r.dkv_all[0] = jnp.concatenate(grad_k, axis=-1)
        r.dkv_all[1] = jnp.concatenate(grad_v, axis=-1)
        r.dkv_out[s] = r.dkv_all[:, row_block(1 - c, local)].astype(LOW)
        dkv_copy(s).start()
        grad_q = jnp.concatenate(grad_q, axis=-1).astype(LOW)
        r.dqkv[s, 0] = grad_q.reshape(r.dqkv.shape[2:])
        r.norm_part[s, 7:8, :head_width] = column_sum(grad_q)
        dkv_copy(s).wait_recv()
        for which in range(2):
            joined = r.dkv_all[which, my_half] + r.dkv_in[s, which].astype(F32)
            joined = joined.astype(LOW)
            r.dqkv[s, 1 + which] = joined.reshape(r.dqkv.shape[2:])
            if which == 1:
                r.norm_part[s, 7:8, half_width : half_width + head_width] = column_sum(joined)

    def leave_back(s, j):
        product = dot_nn(r.dqkv[s, 0, j], r.wq[s, 0:head_width])
        for which in range(1, 3):
            weight = r.wq[s, which * head_width : (which + 1) * head_width]
            product = product + dot_nn(r.dqkv[s, which, j], weight)
        scatter_start(s, 3, j, product)

    @on_owner
    def finish_back(s, j):
        grad = scatter_sum(s, 3, j)
        xhat = r.xhat1[s, j]
        result = r.middle[j] + standard_back(
            grad * r.small[s, 0:1], xhat, r.inv1[s, j, :, 0:1]
        )
        r.upstream[j] = result.astype(LOW)
        keep_rows(r.grad_low, s, j, result.astype(LOW))
        r.norm_part[s, 0:1] += column_sum(grad * xhat)
        r.norm_part[s, 1:2] += column_sum(grad)

    for j in streams:
        turn(lines - 1, j)

    def backward(index, _):
        s = lines - 1 - index
        for j in streams:
            feed_back(s, j)
        rows_start(UPS, s)
        rows_start(GPRE, s)

        @pl.when(index == 1)
        def _():
            share(ACT)
            share(MIX)

        for j in streams:
            between_back(s, j)
            scatter_sent(s, 2, j)
        for j in streams:
            mixed_back(s, j)
        rows_start(BRN, s)
        attend_line_back(s)
        for j in streams:
            leave_back(s, j)
        rows_start(DQKV, s)
        for j in streams:
            finish_back(s, j)
            scatter_sent(s, 3, j)

            @pl.when(s > 0)
            def _():
                turn(s - 1, j)

        norm_start(s)
        home_start(grad_home, s)
        return 0

    lax.fori_loop(0, lines, backward, 0)

    share(GPRE)
    share(DQKV)

    drain(r.norm_all, r.norm_r)
    slot = c * chips + t
    norm_sum = r.norm_all[0]
    for line in range(1, lines):
        norm_sum = norm_sum + r.norm_all[line]
    r.ends[slot] = norm_sum

    def ends_copy(step):
        core, chip = step // chips, step % chips
        view = r.ends.at[slot]
        return remote(
            view,
            view,
            r.ends_s.at[step - 1],
            r.ends_r,
            seq=(c + core) % 2,
            tensor=(t + chip) % chips,
        )

    for step in range(1, 2 * chips):
        ends_copy(step).start()

    for index in range(ACT):
        drain(all_rows[index], r.rows_r.at[index])
    for index in range(ACT, 8):
        share_copy(index, 1 - c).wait_recv()
        share_copy(index, c).wait_send()
    drain(r.acts, r.out_r)
    drain(r.grads, r.grad_r)
    drain(r.ends.at[0 : 2 * chips - 1], r.ends_r)
    for step in range(1, 2 * chips):
        ends_copy(step).wait_send()
    for step in range(1, lines):
        small_copy(step - 1, (a + step) % lines, a).wait_send()
        count_copy(step - 1, (a + step) % lines, a).wait_send()
    for p in range(4):
        for which, line in enumerate((beside(a), above(a))):
            first_hop(p, a, line, which).wait_send()

    @pl.when(end_chip)
    def _():
        first_copy().wait_send()

    def sent(s, _):
        home_sent(out_home, s)
        home_sent(grad_home, s)

        @pl.when(a != s)
        def _():
            norm_copy(s).wait_send()

        kv_copy(s, c).wait_send()
        dkv_copy(s).wait_send()
        for index in range(8):
            rows_sent(index, s)
        for p in range(4):

            @pl.when((a == beside(s)) | (a == above(s)))
            def _():
                second_hop(p, s, 0).wait_send()

            @pl.when(a != s)
            def _():
                core_hop(p, s, c).wait_send()

        return 0

    lax.fori_loop(0, lines, sent, 0)


def relay_call(inputs, cotangent, lengths, chosen, singles, weights):
    lines = lax.axis_size("section")
    chips = lax.axis_size("tensor")
    rows, buckets, width = inputs.shape[1:]
    local, total, half = rows * chips, 2 * rows * chips, width // 2
    head_width, units = weights["wo_in"].shape[0], weights["wp_in"].shape[0]
    heads = head_width // HDIM
    sub, stream = rows // STREAMS, local // STREAMS
    peers, owned = chips - 1, 2 * sub
    vmem, dma = pltpu.VMEM, pltpu.SemaphoreType.DMA
    operands = dict(
        inputs=inputs,
        cotangent=cotangent,
        lengths=lengths,
        chosen=chosen,
        **singles,
        **weights,
    )

    def space(name):
        if name in weights:
            return pl.ANY
        return pltpu.SMEM if operands[name] is lengths else pltpu.VMEM

    sums = dict(
        acts=((lines, rows, width), LOW),
        grads=((lines, rows, width), LOW),
        ends=((2 * chips, 8, width), F32),
    )
    gathered = dict(
        all_nrm=((lines, 2, STREAMS, stream, half), LOW),
        all_nmlp=((lines, 2, STREAMS, stream, half), LOW),
        all_ups=((lines, 2, STREAMS, stream, half), LOW),
        all_brn=((lines, 2, STREAMS, stream, half), LOW),
        all_act=((lines, 2, STREAMS, stream, units), LOW),
        all_gpre=((lines, 2, STREAMS, stream, units), LOW),
        all_mix=((lines, 2, STREAMS, stream, head_width), LOW),
        all_dqkv=((lines, 2, 3, STREAMS, stream, head_width), LOW),
    )
    outputs = dict(**sums, **gathered)
    scratch = dict(
        wq=vmem((lines,) + weights["wq_in"].shape, LOW),
        wo=vmem((lines,) + weights["wo_in"].shape, LOW),
        wf=vmem((lines,) + weights["wf_in"].shape, LOW),
        wp=vmem((lines,) + weights["wp_in"].shape, LOW),
        small_own=vmem((8, width), F32),
        small=vmem((lines, 8, width), F32),
        count_own=vmem((lines, 8, total), F32),
        count=vmem((lines, 8, total), F32),
        hidden=vmem((STREAMS, owned, width), F32),
        middle=vmem((STREAMS, owned, width), F32),
        upstream=vmem((STREAMS, owned, width), LOW),
        first_out=vmem((2, rows, width), LOW),
        first_in=vmem((2, rows, width), LOW),
        xhat1=vmem((lines, STREAMS, owned, width), F32),
        inv1=vmem((lines, STREAMS, owned, 128), F32),
        xhat2=vmem((lines, STREAMS, owned, width), F32),
        inv2=vmem((lines, STREAMS, owned, 128), F32),
        nrm=vmem((lines, STREAMS, stream, width), LOW),
        nmlp=vmem((lines, STREAMS, stream, width), LOW),
        ups=vmem((lines, STREAMS, stream, width), LOW),
        brn=vmem((lines, STREAMS, stream, width), LOW),
        act=vmem((lines, STREAMS, stream, units), LOW),
        gpre=vmem((lines, STREAMS, stream, units), LOW),
        slope=vmem((lines, STREAMS, stream, units), F32),
        mix=vmem((lines, STREAMS, stream, head_width), LOW),
        qry=vmem((lines, STREAMS, stream, head_width), LOW),
        gmix=vmem((STREAMS, stream, head_width), LOW),
        dqkv=vmem((lines, 3, STREAMS, stream, head_width), LOW),
        kv=vmem((lines, 2, total, head_width), LOW),
        soft=vmem((lines, heads, local, total), F32),
        dkv_all=vmem((2, total, head_width), F32),
        dkv_out=vmem((lines, 2, local, head_width), LOW),
        dkv_in=vmem((lines, 2, local, head_width), LOW),
        part=vmem((4, STREAMS, stream, width), LOW),
        arrived=vmem((lines, 4, STREAMS, peers, owned, width), LOW),
        out_low=vmem((lines, 2, rows, width), LOW),
        grad_low=vmem((lines, 2, rows, width), LOW),
        norm_part=vmem((lines, 8, width), F32),
        norm_all=vmem((lines, 8, width), F32),
        w_first_s=dma((4, 2)),
        w_first_r=dma((lines, 4)),
        w_second_s=dma((lines, 4)),
        w_second_r=dma((lines, 4, 2)),
        w_core_s=dma((lines, 4)),
        w_core_r=dma((lines, 4)),
        w_own=dma((4,)),
        small_s=dma((lines - 1,)),
        small_r=dma((lines,)),
        count_s=dma((lines - 1,)),
        count_r=dma((lines,)),
        ag_s=dma((4, STREAMS, peers)),
        ag_r=dma((4, STREAMS, peers)),
        rs_s=dma((4, STREAMS, peers)),
        rs_r=dma((4, STREAMS, peers)),
        kv_s=dma((lines,)),
        kv_r=dma((lines,)),
        dkv_s=dma((lines,)),
        dkv_r=dma((lines,)),
        rows_s=dma((8, lines, 2)),
        rows_r=dma((8,)),
        share_s=dma((4,)),
        share_r=dma((4,)),
        first_s=dma,
        first_r=dma,
        out_s=dma((lines, 2)),
        out_r=dma,
        grad_s=dma((lines, 2)),
        grad_r=dma,
        norm_s=dma((lines,)),
        norm_r=dma,
        ends_s=dma((2 * chips - 1,)),
        ends_r=dma,
    )
    names = tuple(operands) + tuple(outputs) + tuple(scratch)
    results = pl.pallas_call(
        functools.partial(relay_kernel, names),
        out_shape=[jax.ShapeDtypeStruct(shape, kind) for shape, kind in outputs.values()],
        in_specs=[pl.BlockSpec(memory_space=space(name)) for name in operands],
        out_specs=[
            pl.BlockSpec(memory_space=pl.ANY if name in gathered else pltpu.VMEM)
            for name in outputs
        ],
        scratch_shapes=list(scratch.values()),
        compiler_params=pltpu.CompilerParams(
            collective_id=0, has_side_effects=True, vmem_limit_bytes=60 * 2**20
        ),
        name="relay",
    )(*operands.values())
    return dict(zip(outputs, results))


def weights_kernel(names, *refs):
    r = types.SimpleNamespace(**dict(zip(names, refs)))
    step = pl.program_id(0)
    micro_count, rows, buckets, width = r.activations.shape
    chips, units, head_width = r.ends.shape[0] // 2, r.all_act.shape[-1], r.all_mix.shape[-1]

    @pl.when(step == 0)
    def _():
        sums = r.ends[0]
        for other in range(1, 2 * chips):
            sums = sums + r.ends[other]
        singles = (r.ln1_gain, r.ln1_shift, r.ln2_gain, r.ln2_shift, r.b_out, r.b_proj)
        for place, single in enumerate(singles):
            single[...] = sums[place : place + 1]
        for chip in range(chips):
            both = r.ends[chip] + r.ends[chips + chip]
            r.b_fc[:, chip * units : (chip + 1) * units] = both[6:7, :units]
            here = slice(chip * head_width, (chip + 1) * head_width)
            r.b_qv[0:1, here] = both[7:8, :head_width]
            r.b_qv[1:2, here] = both[7:8, width // 2 : width // 2 + head_width]
        for target, source in ((r.activations, r.acts), (r.in_grads, r.grads)):
            for micro in range(micro_count):
                rows_of = [
                    source[micro * buckets + bucket].astype(F32)[:, None, :]
                    for bucket in range(buckets)
                ]
                target[micro] = jnp.concatenate(rows_of, axis=1).astype(LOW)
        for target in (r.w_qkv, r.w_out, r.w_fc, r.w_proj):
            target[...] = jnp.zeros_like(target)

    def rows_of_sequence(ref):
        return ref[0].reshape(2 * chips * rows, ref.shape[-1])

    nrm, nmlp, ups, brn, act, gpre, mix = (
        rows_of_sequence(ref)
        for ref in (r.all_nrm, r.all_nmlp, r.all_ups, r.all_brn, r.all_act, r.all_gpre, r.all_mix)
    )
    r.w_proj[...] += dot_tn(act, ups)
    r.w_fc[...] += dot_tn(nmlp, gpre)
    r.w_out[...] += dot_tn(mix, brn)
    for which in range(3):
        grad = r.all_dqkv[0, :, which].reshape(2 * chips * rows, head_width)
        r.w_qkv[which] += dot_tn(grad, nrm)


def weights_call(relayed, inputs_shape, head_width, units):
    lines = lax.axis_size("section")
    chips = lax.axis_size("tensor")
    width = inputs_shape[-1]
    half = width // 2
    outputs = dict(
        activations=(inputs_shape, LOW),
        in_grads=(inputs_shape, LOW),
        ln1_gain=((1, width), F32),
        ln1_shift=((1, width), F32),
        w_qkv=((3, head_width, half), F32),
        b_qv=((2, width), F32),
        w_out=((head_width, half), F32),
        b_out=((1, width), F32),
        ln2_gain=((1, width), F32),
        ln2_shift=((1, width), F32),
        w_fc=((half, units), F32),
        b_fc=((1, chips * units), F32),
        w_proj=((units, half), F32),
        b_proj=((1, width), F32),
    )

    def spec(array):
        if len(array.shape) < 5:
            return pl.BlockSpec(array.shape, lambda step: (0,) * len(array.shape))
        return pl.BlockSpec(
            (1,) + array.shape[1:], lambda step: (step,) + (0,) * (len(array.shape) - 1)
        )

    def whole(shape):
        return pl.BlockSpec(shape, lambda step: (0,) * len(shape))

    return pl.pallas_call(
        functools.partial(weights_kernel, tuple(relayed) + tuple(outputs)),
        out_shape=[jax.ShapeDtypeStruct(shape, kind) for shape, kind in outputs.values()],
        grid=(lines,),
        in_specs=[spec(array) for array in relayed.values()],
        out_specs=[whole(shape) for shape, _ in outputs.values()],
        compiler_params=pltpu.CompilerParams(vmem_limit_bytes=60 * 2**20),
        name="weight_gradients",
    )(*relayed.values())


def on_line(
    inputs,
    cotangent,
    lengths,
    chosen,
    ln1_gain,
    ln1_shift,
    w_qkv,
    b_qv,
    w_out,
    b_out,
    ln2_gain,
    ln2_shift,
    w_fc,
    b_fc,
    w_proj,
    b_proj,
):
    head_width, units = w_out.shape[1], w_fc.shape[2]
    singles = dict(
        ln1_gain=ln1_gain,
        ln1_shift=ln1_shift,
        ln2_gain=ln2_gain,
        ln2_shift=ln2_shift,
        b_out=b_out,
        b_proj=b_proj,
        b_fc=b_fc,
        b_qv=b_qv[0],
    )
    weights = dict(
        wq_in=jnp.swapaxes(w_qkv[0], 1, 2).reshape(-1, inputs.shape[-1]),
        wo_in=w_out[0],
        wf_in=w_fc[0],
        wp_in=w_proj[0],
    )
    picks = chosen.reshape((-1,) + chosen.shape[-2:])
    relayed = relay_call(inputs, cotangent, lengths, picks, singles, weights)
    results = list(weights_call(relayed, inputs.shape, head_width, units))
    results[4] = jnp.swapaxes(results[4], 1, 2)
    vectors = (2, 3, 7, 8, 9, 11, 13)
    return tuple(
        result if place in vectors else result[None] for place, result in enumerate(results)
    )


def fits_lines(mesh):
    return mesh.shape["section"] == 4 and mesh.shape["seq"] == 2 and mesh.shape["tensor"] == 4


def solution(mesh):
    placed = (
        P(None, ("seq", "tensor"), None, None),
        P(None, ("seq", "tensor"), None, None),
        P(),
        P("section", None, None, "tensor", "seq", None),
        P("section", None),
        P("section", None),
        P("section", None, None, "tensor"),
        P("section", None, "tensor"),
        P("section", "tensor", None),
        P("section", None),
        P("section", None),
        P("section", None),
        P("section", None, "tensor"),
        P("section", "tensor"),
        P("section", "tensor", None),
        P("section", None),
    )
    return jax.shard_map(
        on_line if fits_lines(mesh) else on_device,
        mesh=mesh,
        in_specs=placed,
        out_specs=(
            P("section", None, ("seq", "tensor"), None, None),
            P("section", None, ("seq", "tensor"), None, None),
            P("section", None),
            P("section", None),
            P("section", None, "seq", "tensor"),
            P("section", None, None),
            P("section", "tensor", "seq"),
            P("section", None),
            P("section", None),
            P("section", None),
            P("section", "seq", "tensor"),
            P("section", None),
            P("section", "tensor", "seq"),
            P("section", None),
        ),
        check_vma=False,
    )
```

```python
import functools
import types

import jax
import jax.numpy as jnp
from jax import lax
from jax.experimental import pallas as pl
from jax.experimental.pallas import tpu as pltpu
from jax.sharding import PartitionSpec as P

HDIM = 64
WIN = 64
QB = 64
KSEL = 64


NORM_EPS = 1e-05
MASKED = -1000000000.0


def from_behind(value, axis, steps):
    count = lax.axis_size(axis)
    first, last = (max(0, -steps), min(count, count - steps))
    return lax.ppermute(value, axis, [(source, source + steps) for source in range(first, last)])


def layer_norm(values, gain, shift):
    average = jnp.mean(values, axis=-1, keepdims=True)
    centred = values - average
    variance = jnp.mean(centred * centred, axis=-1, keepdims=True)
    return centred * lax.rsqrt(variance + NORM_EPS) * gain + shift


def gelu_tanh(values):
    return (
        0.5
        * values
        * (1.0 + jnp.tanh(0.7978845608028654 * (values + 0.044715 * values * values * values)))
    )


def gather_rows(row_block):
    return lax.all_gather(row_block, "tensor", axis=0, tiled=True)


def scatter_product(left_rows, weight, formula):
    return lax.psum_scatter(
        jnp.einsum(formula, left_rows, weight, preferred_element_type=jnp.float32).astype(
            jnp.bfloat16
        ),
        "tensor",
        scatter_dimension=0,
        tiled=True,
    ).astype(jnp.float32)


def near_slabs(full_rows, seq_start, seq_first, length_local):
    buckets = full_rows.shape[1]
    heads_local = full_rows.shape[2] // HDIM
    blocks = length_local // QB
    earlier = lax.dynamic_slice_in_dim(full_rows, jnp.maximum(seq_start - WIN, 0), WIN, 0)
    earlier = jnp.where(seq_first, jnp.zeros_like(earlier), earlier)
    local_part = lax.dynamic_slice_in_dim(full_rows, seq_start, length_local, 0)
    segment = jnp.concatenate([earlier, local_part], 0).reshape(
        length_local + WIN, buckets, heads_local, HDIM
    )
    return jnp.concatenate(
        [
            segment[offset_index * QB : offset_index * QB + length_local].reshape(
                blocks, QB, buckets, heads_local, HDIM
            )
            for offset_index in range(WIN // QB + 1)
        ],
        1,
    )


def far_rows(full_rows, flat_index):
    total_rows, buckets, feature_width = full_rows.shape
    heads_local = feature_width // HDIM
    return jnp.take(full_rows.reshape(total_rows * buckets * heads_local, HDIM), flat_index, axis=0)


def key_geometry(chosen_now, seq_start, blocks):
    buckets, heads_local = (chosen_now.shape[0], chosen_now.shape[1])
    bucket_ids = lax.broadcasted_iota(jnp.int32, chosen_now.shape, 0)
    head_ids = lax.broadcasted_iota(jnp.int32, chosen_now.shape, 1)
    flat_index = (chosen_now * buckets + bucket_ids) * heads_local + head_ids
    block_start = seq_start + QB * lax.broadcasted_iota(jnp.int32, (blocks, 1, 1), 0)
    query_ids = lax.broadcasted_iota(jnp.int32, (1, QB, 1), 1)
    key_ids = lax.broadcasted_iota(jnp.int32, (1, 1, WIN + QB), 2)
    distance = query_ids + WIN - key_ids
    near_ok = (distance >= 0) & (distance < WIN) & (block_start + key_ids - WIN >= 0)
    far_ok = chosen_now + WIN <= block_start.reshape(1, 1, blocks, 1)
    near_mask = jnp.broadcast_to(
        near_ok[:, None, None], (blocks, buckets, heads_local, QB, WIN + QB)
    )
    far_mask = jnp.broadcast_to(
        jnp.transpose(far_ok, (2, 0, 1, 3))[:, :, :, None, :],
        (blocks, buckets, heads_local, QB, KSEL),
    )
    return (flat_index, jnp.concatenate([near_mask, far_mask], -1))


def attention_setup(queries, key_rows, value_rows, chosen_now, seq_start, seq_first):
    length_local, buckets, feature_width = queries.shape
    heads_local = feature_width // HDIM
    blocks = length_local // QB
    query_blocks = queries.reshape(blocks, QB, buckets, heads_local, HDIM)
    flat_index, key_mask = key_geometry(chosen_now, seq_start, blocks)
    near_keys = near_slabs(key_rows, seq_start, seq_first, length_local)
    near_values = near_slabs(value_rows, seq_start, seq_first, length_local)
    far_keys = far_rows(key_rows, flat_index)
    far_values = far_rows(value_rows, flat_index)
    near_scores = jnp.einsum(
        "bqnhe,btnhe->bnhqt", query_blocks, near_keys, preferred_element_type=jnp.float32
    )
    far_scores = jnp.einsum(
        "bqnhe,nhbke->bnhqk", query_blocks, far_keys, preferred_element_type=jnp.float32
    )
    scores = jnp.where(
        key_mask, HDIM ** (-0.5) * jnp.concatenate([near_scores, far_scores], -1), MASKED
    )
    return (query_blocks, near_keys, near_values, far_keys, far_values, flat_index, scores)


def attend(queries, key_rows, value_rows, chosen_now, seq_start, seq_first):
    query_blocks, near_keys, near_values, far_keys, far_values, flat_index, scores = (
        attention_setup(queries, key_rows, value_rows, chosen_now, seq_start, seq_first)
    )
    span = WIN + QB
    row_top = jnp.max(scores, -1, keepdims=True)
    exp_terms = jnp.exp(scores - row_top)
    row_total = jnp.sum(exp_terms, -1, keepdims=True)
    softmax_low = (exp_terms / row_total).astype(jnp.bfloat16)
    near_part = jnp.einsum(
        "bnhqt,btnhe->bqnhe",
        softmax_low[..., :span],
        near_values,
        preferred_element_type=jnp.float32,
    )
    far_part = jnp.einsum(
        "bnhqk,nhbke->bqnhe",
        softmax_low[..., span:],
        far_values,
        preferred_element_type=jnp.float32,
    )
    return ((near_part + far_part).reshape(queries.shape), row_top + jnp.log(row_total))


def spread_back(near_grad, far_grad, flat_index, seq_start, seq_first, total_rows):
    blocks, span, buckets, heads_local, head_size = near_grad.shape
    length_local = blocks * QB
    feature_width = heads_local * head_size
    segment = jnp.zeros((length_local + WIN, buckets, heads_local, head_size), jnp.float32)
    for offset_index in range(WIN // QB + 1):
        piece = near_grad[:, offset_index * QB : (offset_index + 1) * QB].reshape(
            length_local, buckets, heads_local, head_size
        )
        segment = segment.at[offset_index * QB : offset_index * QB + length_local].add(piece)
    full_rows = jnp.zeros((total_rows * buckets * heads_local, head_size), jnp.float32)
    full_rows = full_rows.at[flat_index.reshape(-1)].add(far_grad.reshape(-1, head_size))
    full_rows = full_rows.reshape(total_rows, buckets, feature_width)
    local_part = segment[WIN:].reshape(length_local, buckets, feature_width)
    earlier = jnp.where(seq_first, 0.0, segment[:WIN].reshape(WIN, buckets, feature_width))
    full_rows = lax.dynamic_update_slice_in_dim(
        full_rows,
        lax.dynamic_slice_in_dim(full_rows, seq_start, length_local, 0) + local_part,
        seq_start,
        0,
    )
    earlier_start = jnp.maximum(seq_start - WIN, 0)
    full_rows = lax.dynamic_update_slice_in_dim(
        full_rows,
        lax.dynamic_slice_in_dim(full_rows, earlier_start, WIN, 0) + earlier,
        earlier_start,
        0,
    )
    return full_rows


def attend_back(
    queries, key_rows, value_rows, chosen_now, seq_start, seq_first, log_total, grad_mixed
):
    query_blocks, near_keys, near_values, far_keys, far_values, flat_index, scores = (
        attention_setup(queries, key_rows, value_rows, chosen_now, seq_start, seq_first)
    )
    span = WIN + QB
    score_scale = HDIM ** (-0.5)
    grad_blocks = grad_mixed.reshape(query_blocks.shape)
    weights_full = jnp.exp(scores - log_total)
    softmax_low = weights_full.astype(jnp.bfloat16)
    grad_near_weights = jnp.einsum(
        "bqnhe,btnhe->bnhqt", grad_blocks, near_values, preferred_element_type=jnp.float32
    )
    grad_far_weights = jnp.einsum(
        "bqnhe,nhbke->bnhqk", grad_blocks, far_values, preferred_element_type=jnp.float32
    )
    grad_weights = jnp.concatenate([grad_near_weights, grad_far_weights], -1)
    row_dot = jnp.sum(weights_full * grad_weights, -1, keepdims=True)
    grad_scores = (weights_full * (grad_weights - row_dot)).astype(jnp.bfloat16)
    grad_near, grad_far = (grad_scores[..., :span], grad_scores[..., span:])
    grad_queries = score_scale * (
        jnp.einsum("bnhqt,btnhe->bqnhe", grad_near, near_keys, preferred_element_type=jnp.float32)
        + jnp.einsum("bnhqk,nhbke->bqnhe", grad_far, far_keys, preferred_element_type=jnp.float32)
    )
    near_key_grad = score_scale * jnp.einsum(
        "bnhqt,bqnhe->btnhe", grad_near, query_blocks, preferred_element_type=jnp.float32
    )
    far_key_grad = score_scale * jnp.einsum(
        "bnhqk,bqnhe->nhbke", grad_far, query_blocks, preferred_element_type=jnp.float32
    )
    near_value_grad = jnp.einsum(
        "bnhqt,bqnhe->btnhe",
        softmax_low[..., :span],
        grad_blocks,
        preferred_element_type=jnp.float32,
    )
    far_value_grad = jnp.einsum(
        "bnhqk,bqnhe->nhbke",
        softmax_low[..., span:],
        grad_blocks,
        preferred_element_type=jnp.float32,
    )
    total_rows = key_rows.shape[0]
    key_grad = spread_back(
        near_key_grad, far_key_grad, flat_index, seq_start, seq_first, total_rows
    )
    value_grad = spread_back(
        near_value_grad, far_value_grad, flat_index, seq_start, seq_first, total_rows
    )
    return (grad_queries.reshape(queries.shape), key_grad, value_grad)


def forward_pass(hidden, params, chosen_now, query_mask, seq_start, seq_first, finish):
    (
        ln1_gain,
        ln1_shift,
        w_qkv,
        b_qv,
        w_out,
        b_out,
        ln2_gain,
        ln2_shift,
        w_fc,
        b_fc,
        w_proj,
        b_proj,
    ) = params
    hidden_wide = hidden.astype(jnp.float32)
    normed_all = gather_rows(layer_norm(hidden_wide, ln1_gain, ln1_shift).astype(jnp.bfloat16))
    projected = jnp.einsum("pnd,jdc->jpnc", normed_all, w_qkv, preferred_element_type=jnp.float32)
    queries = (projected[0] + b_qv[0]).astype(jnp.bfloat16)
    key_rows, value_rows = (
        lax.all_gather(projected[1].astype(jnp.bfloat16), "seq", axis=0, tiled=True),
        lax.all_gather((projected[2] + b_qv[1]).astype(jnp.bfloat16), "seq", axis=0, tiled=True),
    )
    attended, log_total = attend(queries, key_rows, value_rows, chosen_now, seq_start, seq_first)
    mixed_rows = (attended * query_mask[:, :, None]).astype(jnp.bfloat16)
    middle = hidden_wide + scatter_product(mixed_rows, w_out, "pnc,cd->pnd") + b_out
    normed_mlp = gather_rows(layer_norm(middle, ln2_gain, ln2_shift).astype(jnp.bfloat16))
    pre_active = (
        jnp.einsum("pnd,df->pnf", normed_mlp, w_fc, preferred_element_type=jnp.float32) + b_fc
    )
    active = gelu_tanh(pre_active).astype(jnp.bfloat16)
    if not finish:
        return (
            normed_all,
            queries,
            key_rows,
            value_rows,
            log_total,
            mixed_rows,
            middle,
            normed_mlp,
            pre_active,
            active,
        )
    output = (middle + scatter_product(active, w_proj, "pnf,fd->pnd") + b_proj).astype(jnp.bfloat16)
    return (output, (key_rows, value_rows))


def backward_pass(hidden, upstream, params, chosen_now, query_mask, seq_start, seq_first):
    (
        ln1_gain,
        ln1_shift,
        w_qkv,
        b_qv,
        w_out,
        b_out,
        ln2_gain,
        ln2_shift,
        w_fc,
        b_fc,
        w_proj,
        b_proj,
    ) = params
    (
        normed_all,
        queries,
        key_rows,
        value_rows,
        log_total,
        mixed_rows,
        middle,
        normed_mlp,
        pre_active,
        active,
    ) = forward_pass(hidden, params, chosen_now, query_mask, seq_start, seq_first, False)
    upstream_all = gather_rows(upstream)
    grad_w_proj = jnp.einsum(
        "pnf,pnd->fd", active, upstream_all, preferred_element_type=jnp.float32
    )
    grad_b_proj = jnp.sum(upstream.astype(jnp.float32), axis=(0, 1))
    grad_active = jnp.einsum(
        "pnd,fd->pnf", upstream_all, w_proj, preferred_element_type=jnp.float32
    )
    unused_value, gelu_pull = jax.vjp(gelu_tanh, pre_active)
    grad_pre = gelu_pull(grad_active)[0].astype(jnp.bfloat16)
    grad_w_fc = jnp.einsum("pnd,pnf->df", normed_mlp, grad_pre, preferred_element_type=jnp.float32)
    grad_b_fc = jnp.sum(grad_pre.astype(jnp.float32), axis=(0, 1))
    grad_normed_mlp = scatter_product(grad_pre, w_fc, "pnf,df->pnd")
    unused_norm, second_pull = jax.vjp(layer_norm, middle, ln2_gain, ln2_shift)
    grad_mid_norm, grad_ln2_gain, grad_ln2_shift = second_pull(grad_normed_mlp)
    grad_middle = upstream.astype(jnp.float32) + grad_mid_norm
    grad_branch = grad_middle.astype(jnp.bfloat16)
    grad_b_out = jnp.sum(grad_branch.astype(jnp.float32), axis=(0, 1))
    branch_all = gather_rows(grad_branch)
    grad_w_out = jnp.einsum(
        "pnc,pnd->cd", mixed_rows, branch_all, preferred_element_type=jnp.float32
    )
    grad_mixed = jnp.einsum(
        "pnd,cd->pnc", branch_all, w_out, preferred_element_type=jnp.float32
    ).astype(jnp.bfloat16) * query_mask[:, :, None].astype(jnp.bfloat16)
    grad_queries, key_grad_all, value_grad_all = attend_back(
        queries, key_rows, value_rows, chosen_now, seq_start, seq_first, log_total, grad_mixed
    )
    key_grad, value_grad = (
        lax.psum_scatter(
            key_grad_all.astype(jnp.bfloat16), "seq", scatter_dimension=0, tiled=True
        ).astype(jnp.float32),
        lax.psum_scatter(
            value_grad_all.astype(jnp.bfloat16), "seq", scatter_dimension=0, tiled=True
        ).astype(jnp.float32),
    )
    grad_project = jnp.stack(
        [
            grad_queries.astype(jnp.bfloat16),
            key_grad.astype(jnp.bfloat16),
            value_grad.astype(jnp.bfloat16),
        ],
        2,
    )
    grad_w_qkv = jnp.einsum(
        "pnd,pnjc->jdc", normed_all, grad_project, preferred_element_type=jnp.float32
    )
    grad_b_qv = jnp.sum(grad_project[:, :, 0::2].astype(jnp.float32), axis=(0, 1))
    grad_normed = scatter_product(grad_project, w_qkv, "pnjc,jdc->pnd")
    unused_first, first_pull = jax.vjp(layer_norm, hidden.astype(jnp.float32), ln1_gain, ln1_shift)
    grad_in_norm, grad_ln1_gain, grad_ln1_shift = first_pull(grad_normed)
    grad_hidden = (grad_middle + grad_in_norm).astype(jnp.bfloat16)
    block_grads = (
        grad_ln1_gain,
        grad_ln1_shift,
        grad_w_qkv,
        grad_b_qv,
        grad_w_out,
        grad_b_out,
        grad_ln2_gain,
        grad_ln2_shift,
        grad_w_fc,
        grad_b_fc,
        grad_w_proj,
        grad_b_proj,
    )
    return (grad_hidden, block_grads)


def on_device(
    inputs,
    cotangent,
    lengths,
    chosen,
    ln1_gain,
    ln1_shift,
    w_qkv,
    b_qv,
    w_out,
    b_out,
    ln2_gain,
    ln2_shift,
    w_fc,
    b_fc,
    w_proj,
    b_proj,
):
    params = tuple(
        (
            weight_array[0]
            for weight_array in (
                ln1_gain,
                ln1_shift,
                w_qkv,
                b_qv,
                w_out,
                b_out,
                ln2_gain,
                ln2_shift,
                w_fc,
                b_fc,
                w_proj,
                b_proj,
            )
        )
    )
    section_index = lax.axis_index("section")
    section_count = lax.axis_size("section")
    seq_index = lax.axis_index("seq")
    tensor_index = lax.axis_index("tensor")
    tensor_count = lax.axis_size("tensor")
    micro_count, rows_local, buckets, feature_width = inputs.shape
    length_local = rows_local * tensor_count
    heads_width = w_qkv.shape[-1]
    seq_start = seq_index * length_local
    seq_first = seq_index == 0
    positions = seq_start + lax.broadcasted_iota(jnp.int32, (micro_count, length_local, buckets), 1)
    mask_all = (positions < lengths[:, None, :]).astype(jnp.float32)
    mask_rows = lax.dynamic_slice_in_dim(mask_all, tensor_index * rows_local, rows_local, 1)
    step_count = micro_count + section_count - 1
    chosen_section = chosen[0]
    received = jnp.zeros((rows_local, buckets, feature_width), jnp.bfloat16)
    stored = jnp.zeros((micro_count, rows_local, buckets, feature_width), jnp.bfloat16)
    outputs = jnp.zeros_like(stored)
    for step_index in range(step_count):
        micro_index = step_index - section_index
        running = (micro_index >= 0) & (micro_index < micro_count)
        slot_index = jnp.clip(micro_index, 0, micro_count - 1)
        block_in = jnp.where(
            section_index == 0, lax.dynamic_index_in_dim(inputs, slot_index, 0, False), received
        )
        chosen_now = lax.dynamic_index_in_dim(chosen_section, slot_index, 0, False)
        query_mask = lax.dynamic_index_in_dim(mask_all, slot_index, 0, False)
        result, key_pair = forward_pass(
            block_in, params, chosen_now, query_mask, seq_start, seq_first, True
        )
        stored = jnp.where(
            running, lax.dynamic_update_index_in_dim(stored, block_in, slot_index, 0), stored
        )
        outputs = jnp.where(
            running, lax.dynamic_update_index_in_dim(outputs, result, slot_index, 0), outputs
        )
        received = from_behind(result, "section", 1)
    back_received = jnp.zeros((rows_local, buckets, feature_width), jnp.bfloat16)
    in_grads = jnp.zeros_like(stored)
    totals = None
    for step_index in range(step_count):
        micro_index = step_index - (section_count - 1 - section_index)
        running = (micro_index >= 0) & (micro_index < micro_count)
        slot_index = jnp.clip(micro_index, 0, micro_count - 1)
        chosen_now = lax.dynamic_index_in_dim(chosen_section, slot_index, 0, False)
        query_mask = lax.dynamic_index_in_dim(mask_all, slot_index, 0, False)
        local_mask = lax.dynamic_index_in_dim(mask_rows, slot_index, 0, False)
        top_grad = (
            lax.dynamic_index_in_dim(cotangent, slot_index, 0, False).astype(jnp.float32)
            * local_mask[:, :, None]
        ).astype(jnp.bfloat16)
        upstream = jnp.where(section_index == section_count - 1, top_grad, back_received)
        hidden = lax.dynamic_index_in_dim(stored, slot_index, 0, False)
        grad_hidden, block_grads = backward_pass(
            hidden, upstream, params, chosen_now, query_mask, seq_start, seq_first
        )
        block_grads = tuple(
            (jnp.where(running, grad_part, jnp.zeros_like(grad_part)) for grad_part in block_grads)
        )
        totals = (
            block_grads
            if step_index == 0
            else tuple(
                (total_part + grad_part for total_part, grad_part in zip(totals, block_grads))
            )
        )
        in_grads = jnp.where(
            running, lax.dynamic_update_index_in_dim(in_grads, grad_hidden, slot_index, 0), in_grads
        )
        back_received = from_behind(grad_hidden, "section", -1)
    (
        sum_ln1_gain,
        sum_ln1_shift,
        sum_w_qkv,
        sum_b_qv,
        sum_w_out,
        sum_b_out,
        sum_ln2_gain,
        sum_ln2_shift,
        sum_w_fc,
        sum_b_fc,
        sum_w_proj,
        sum_b_proj,
    ) = totals
    part_qkv, part_out, part_fc, part_proj = (
        lax.psum_scatter(
            sum_w_qkv.astype(jnp.bfloat16), "seq", scatter_dimension=1, tiled=True
        ).astype(jnp.float32),
        lax.psum_scatter(
            sum_w_out.astype(jnp.bfloat16), "seq", scatter_dimension=1, tiled=True
        ).astype(jnp.float32),
        lax.psum_scatter(
            sum_w_fc.astype(jnp.bfloat16), "seq", scatter_dimension=0, tiled=True
        ).astype(jnp.float32),
        lax.psum_scatter(
            sum_w_proj.astype(jnp.bfloat16), "seq", scatter_dimension=1, tiled=True
        ).astype(jnp.float32),
    )
    bias_qv = lax.dynamic_update_slice_in_dim(
        jnp.zeros((2, feature_width), jnp.float32), sum_b_qv, tensor_index * heads_width, 1
    )
    units_local = sum_b_fc.shape[0]
    bias_fc = lax.dynamic_update_slice_in_dim(
        jnp.zeros((units_local * tensor_count,), jnp.float32),
        sum_b_fc,
        tensor_index * units_local,
        0,
    )
    small_sums = lax.psum(
        (
            sum_ln1_gain,
            sum_ln1_shift,
            bias_qv,
            sum_b_out,
            sum_ln2_gain,
            sum_ln2_shift,
            bias_fc,
            sum_b_proj,
        ),
        ("seq", "tensor"),
    )
    return (
        outputs[None],
        in_grads[None],
        small_sums[0][None],
        small_sums[1][None],
        part_qkv[None],
        small_sums[2][None],
        part_out[None],
        small_sums[3][None],
        small_sums[4][None],
        small_sums[5][None],
        part_fc[None],
        small_sums[6][None],
        part_proj[None],
        small_sums[7][None],
    )


STREAMS = 2
NRM, NMLP, UPS, BRN, ACT, GPRE, MIX, DQKV = range(8)
F32 = jnp.float32
LOW = jnp.bfloat16
MESH_ID = pl.DeviceIdType.MESH


def dot_nn(left, right):
    return lax.dot_general(left, right, (((1,), (0,)), ((), ())), preferred_element_type=F32)


def dot_nt(left, right):
    return lax.dot_general(left, right, (((1,), (1,)), ((), ())), preferred_element_type=F32)


def dot_tn(left, right):
    return lax.dot_general(left, right, (((0,), (0,)), ((), ())), preferred_element_type=F32)


def standard(rows):
    centred = rows - jnp.mean(rows, axis=-1, keepdims=True)
    scale = lax.rsqrt(jnp.mean(centred * centred, axis=-1, keepdims=True) + NORM_EPS)
    return centred * scale, scale


def standard_back(grad, xhat, scale):
    inner = jnp.mean(grad * xhat, axis=-1, keepdims=True)
    return scale * (grad - jnp.mean(grad, axis=-1, keepdims=True) - xhat * inner)


def column_sum(rows):
    return jnp.sum(rows.astype(F32), axis=0, keepdims=True)


def relay_kernel(names, *refs):
    r = types.SimpleNamespace(**dict(zip(names, refs)))
    a, c, t = (lax.axis_index(name) for name in ("section", "seq", "tensor"))
    lines = lax.axis_size("section")
    chips = lax.axis_size("tensor")
    rows, buckets, width = r.inputs.shape[1:]
    half_width = width // 2
    local = rows * chips
    total = 2 * local
    sub = rows // STREAMS
    stream_rows = local // STREAMS
    head_width = r.wo_in.shape[0]
    heads = head_width // HDIM
    blocks = local // QB
    units = r.wp_in.shape[0]
    scale = HDIM ** (-0.5)
    streams = range(STREAMS)

    def remote(src, dst, send, recv, **target):
        return pltpu.make_async_remote_copy(
            src_ref=src,
            dst_ref=dst,
            send_sem=send,
            recv_sem=recv,
            device_id=target,
            device_id_type=MESH_ID,
        )

    def drain(ref, sem):
        pltpu.make_async_copy(ref, ref, sem).wait()

    def row_block(index, size):
        return pl.ds(pl.multiple_of(index * size, size), size)

    near_chip = t + 1 - 2 * (t % 2)
    over_chip = (t + 2) % 4
    across_chip = 3 - t
    middle_chip = (t == 1) | (t == 2)
    end_chip = (t == 0) | (t == 3)
    owned = 2 * sub
    mine = row_block(t - 1, owned)
    my_half = row_block(c, local)

    barrier = pltpu.get_barrier_semaphore()
    for core in range(2):
        for step in range(1, chips):
            there = {"tensor": (t + step) % chips, "seq": core}
            pl.semaphore_signal(barrier, inc=1, device_id=there, device_id_type=MESH_ID)
        for step in range(1, lines):
            there = {"section": (a + step) % lines, "seq": core}
            pl.semaphore_signal(barrier, inc=1, device_id=there, device_id_type=MESH_ID)
    for step in range(1, lines):
        there = {"section": (a + step) % lines, "tensor": near_chip}
        pl.semaphore_signal(barrier, inc=1, device_id=there, device_id_type=MESH_ID)
    pl.semaphore_signal(barrier, inc=1, device_id={"seq": 1 - c}, device_id_type=MESH_ID)
    pl.semaphore_wait(barrier, 2 * (chips - 1) + 3 * (lines - 1) + 1)

    def beside(s):
        return s + 1 - 2 * (s % 2)

    def above(s):
        return (s + 2) % 4

    def store(p):
        return (r.wq, r.wo, r.wf, r.wp)[p]

    def source(p):
        return (r.wq_in, r.wo_in, r.wf_in, r.wp_in)[p]

    def height(p):
        return source(p).shape[0]

    def core_half(p, s, core):
        return store(p).at[s, row_block(core, height(p) // 2)]

    def first_hop(p, s, neighbour, which):
        return remote(
            source(p).at[row_block(c, height(p) // 2)],
            core_half(p, s, c),
            r.w_first_s.at[p, which],
            r.w_first_r.at[s, p],
            section=neighbour,
        )

    def second_hop(p, s, which):
        view = store(p).at[s, row_block(2 * c + which, height(p) // 4)]
        return remote(
            view, view, r.w_second_s.at[s, p], r.w_second_r.at[s, p, which], section=3 - s
        )

    def core_hop(p, s, core):
        view = core_half(p, s, core)
        return remote(view, view, r.w_core_s.at[s, p], r.w_core_r.at[s, p], seq=1 - c)

    def own_copy(p):
        return pltpu.make_async_copy(source(p), store(p).at[a], r.w_own.at[p])

    def pass_on(s, p, which):
        line = (beside(s), above(s))[which]

        @pl.when(a == line)
        def _():
            first_hop(p, s, line, which).wait_recv()
            second_hop(p, s, which).start()
            core_hop(p, s, c).start()

    def pass_later(pieces, at_first):
        for later in range(1, lines):
            for which in range(2):
                if ((beside(later), above(later))[which] == 0) == at_first:
                    for p in pieces:
                        pass_on(later, p, which)

    def pass_far(s, p):
        @pl.when(a == 3 - s)
        def _():
            second_hop(p, s, 0).wait_recv()
            second_hop(p, s, 1).wait_recv()
            core_hop(p, s, c).start()

    def need(s, p):
        @pl.when(s == 0)
        def _():
            pass_on(0, p, 0)
            pass_on(0, p, 1)
            pass_far(0, p)

        @pl.when(a == s)
        def _():
            own_copy(p).wait()

        @pl.when(a != s)
        def _():
            core_hop(p, s, 1 - c).wait_recv()

    def small_copy(step, line, slot):
        return remote(
            r.small_own, r.small.at[slot], r.small_s.at[step], r.small_r.at[slot], section=line
        )

    def count_copy(step, line, slot):
        return remote(
            r.count_own.at[line],
            r.count.at[slot],
            r.count_s.at[step],
            r.count_r.at[slot],
            section=line,
        )

    singles = (r.ln1_gain, r.ln1_shift, r.ln2_gain, r.ln2_shift, r.b_out, r.b_proj)
    for place, single in enumerate(singles):
        r.small_own[place : place + 1] = single[...]
    r.small_own[6:7, :units] = r.b_fc[...]
    r.small_own[7:8, :head_width] = r.b_qv[0:1]
    r.small_own[7:8, half_width : half_width + head_width] = r.b_qv[1:2]
    for step in range(1, lines):
        small_copy(step - 1, (a + step) % lines, a).start()
    for p in range(4):
        for which, line in enumerate((beside(a), above(a))):
            first_hop(p, a, line, which).start()
    for p in range(4):
        own_copy(p).start()
    r.small[a] = r.small_own[...]

    def place_of(index):
        inside = index % local
        stream, left = inside // stream_rows, inside % stream_rows
        return (index // local) * local + (left // sub) * rows + stream * sub + left % sub

    def iota(shape, dimension):
        return lax.broadcasted_iota(jnp.int32, shape, dimension)

    square = jnp.where(iota((KSEL, KSEL), 0) == iota((KSEL, KSEL), 1), 1.0, 0.0).astype(LOW)
    position = place_of(iota((KSEL, total), 1)).astype(F32)
    for pair in range(lines * heads):
        line, head = pair // heads, pair % heads
        columns = dot_nt(square, r.chosen[pair].astype(F32).astype(LOW))
        for block in range(blocks):
            pick = head * blocks + block
            r.count_own[line, pick : pick + 1, :] = jnp.sum(
                jnp.where(columns[:, block : block + 1] == position, 1.0, 0.0),
                axis=0,
                keepdims=True,
            )
    for step in range(1, lines):
        count_copy(step - 1, (a + step) % lines, a).start()
    r.count[a] = r.count_own[a]

    NEAR, OVER, ACROSS = range(3)

    def gather(buffer, s, kind, j, owner, target, slot):
        view = buffer.at[s, j, row_block(owner - 1, owned)]
        return remote(
            view, view, r.ag_s.at[kind, j, slot], r.ag_r.at[kind, j, slot], tensor=target
        )

    def gather_start(buffer, s, kind, j):
        gather(buffer, s, kind, j, t, over_chip, OVER).start()
        gather(buffer, s, kind, j, t, across_chip, ACROSS).start()
        gather(buffer, s, kind, j, t, near_chip, NEAR).start()

    def gather_wait(buffer, s, kind, j):
        @pl.when(middle_chip)
        def _():
            gather(buffer, s, kind, j, across_chip, across_chip, ACROSS).wait_recv()

        @pl.when(end_chip)
        def _():
            gather(buffer, s, kind, j, near_chip, near_chip, NEAR).wait_recv()
            gather(buffer, s, kind, j, over_chip, over_chip, OVER).wait_recv()

    def gather_sent(buffer, s, kind, j):
        @pl.when(middle_chip)
        def _():
            gather(buffer, s, kind, j, t, over_chip, OVER).wait_send()
            gather(buffer, s, kind, j, t, across_chip, ACROSS).wait_send()
            gather(buffer, s, kind, j, t, near_chip, NEAR).wait_send()

    def scatter(s, kind, j, owner, slot):
        return remote(
            r.part.at[kind, j, row_block(owner - 1, owned)],
            r.arrived.at[s, kind, j, slot],
            r.rs_s.at[kind, j, slot],
            r.rs_r.at[kind, j, slot],
            tensor=owner,
        )

    def scatter_start(s, kind, j, product):
        r.part[kind, j] = product.astype(LOW)

        @pl.when(end_chip)
        def _():
            scatter(s, kind, j, over_chip, OVER).start()
            scatter(s, kind, j, near_chip, NEAR).start()

        @pl.when(middle_chip)
        def _():
            scatter(s, kind, j, across_chip, ACROSS).start()

    def scatter_sum(s, kind, j):
        result = r.part[kind, j, mine].astype(F32)
        for slot in (NEAR, ACROSS, OVER):
            scatter(s, kind, j, t, slot).wait_recv()
            result = result + r.arrived[s, kind, j, slot].astype(F32)
        return result

    def scatter_sent(s, kind, j):
        @pl.when(end_chip)
        def _():
            scatter(s, kind, j, over_chip, OVER).wait_send()
            scatter(s, kind, j, near_chip, NEAR).wait_send()

        @pl.when(middle_chip)
        def _():
            scatter(s, kind, j, across_chip, ACROSS).wait_send()

    own_rows = (r.nrm, r.nmlp, r.ups, r.brn, r.act, r.gpre, r.mix, r.dqkv)
    all_rows = (
        r.all_nrm,
        r.all_nmlp,
        r.all_ups,
        r.all_brn,
        r.all_act,
        r.all_gpre,
        r.all_mix,
        r.all_dqkv,
    )

    def rows_copy(index, s, same, stays=False):
        core = c if same else 1 - c
        src = own_rows[index].at[s]
        dst = all_rows[index].at[a, c]
        if index <= BRN:
            src = src.at[:, :, row_block(core, half_width)]
        recv = r.rows_r.at[index]
        if stays:
            return pltpu.make_async_copy(src, dst, recv)
        if same:
            return remote(src, dst, r.rows_s.at[index, s, 0], recv, section=s)
        return remote(src, dst, r.rows_s.at[index, s, 1], recv, section=s, seq=1 - c)

    def rows_start(index, s):
        @pl.when(a == s)
        def _():
            rows_copy(index, s, True, True).start()

        @pl.when(a != s)
        def _():
            rows_copy(index, s, True).start()

        if index <= BRN:
            rows_copy(index, s, False).start()

    def rows_sent(index, s):
        @pl.when(a != s)
        def _():
            rows_copy(index, s, True).wait_send()

        if index <= BRN:
            rows_copy(index, s, False).wait_send()

    def share_copy(index, core):
        view = all_rows[index].at[:, core]
        return remote(view, view, r.share_s.at[index - ACT], r.share_r.at[index - ACT], seq=1 - c)

    def share(index):
        drain(all_rows[index].at[:, c], r.rows_r.at[index])
        share_copy(index, c).start()

    def norm_copy(s):
        return remote(
            r.norm_part.at[s], r.norm_all.at[a], r.norm_s.at[s], r.norm_r, section=s
        )

    def norm_start(s):
        @pl.when(a == s)
        def _():
            pltpu.make_async_copy(r.norm_part.at[s], r.norm_all.at[a], r.norm_r).start()

        @pl.when(a != s)
        def _():
            norm_copy(s).start()

    def home_copy(what, s, chip):
        src, dst, send, recv = what
        return remote(
            src.at[s, chip % 2],
            dst.at[a],
            send.at[s, chip % 2],
            recv,
            section=s,
            tensor=chip,
        )

    def home_start(what, s):
        src, dst, send, recv = what

        @pl.when(middle_chip & (a == s))
        def _():
            pltpu.make_async_copy(src.at[s, t % 2], dst.at[a], recv).start()

        @pl.when(middle_chip & (a != s))
        def _():
            home_copy(what, s, t).start()

        @pl.when(middle_chip)
        def _():
            home_copy(what, s, near_chip).start()

    def home_sent(what, s):
        @pl.when(middle_chip & (a != s))
        def _():
            home_copy(what, s, t).wait_send()

        @pl.when(middle_chip)
        def _():
            home_copy(what, s, near_chip).wait_send()

    out_home = (r.out_low, r.acts, r.out_s, r.out_r)
    grad_home = (r.grad_low, r.grads, r.grad_s, r.grad_r)

    length = r.lengths[a // buckets, a % buckets]
    key = place_of(iota((stream_rows, total), 1))
    for j in streams:
        query = place_of(c * local + j * stream_rows + iota((stream_rows, total), 0))
        r.near[j] = jnp.where((query >= key) & (query - key < WIN), 1.0, 0.0)
    key_row = place_of(iota((1, total), 1))

    def row_mask(place):
        return jnp.where(place < length, 1.0, 0.0)

    def multiplicity(s, j, head):
        far = []
        for block in range(blocks):
            pick = head * blocks + block
            limit = (c * blocks + block) * QB - WIN
            counted = jnp.where(key_row <= limit, r.count[s, pick : pick + 1, :], 0.0)
            far.append(jnp.broadcast_to(counted, (stream_rows // blocks, total)))
        return r.near[j] + jnp.concatenate(far, axis=0)

    def head_cols(head):
        return slice(head * HDIM, (head + 1) * HDIM)

    def kv_copy(s):
        view = r.kv.at[s, :, 0:local]
        return remote(view, view, r.kv_s.at[s], r.kv_r.at[s], seq=1 - c)

    def dkv_copy(s):
        return remote(r.dkv_out.at[s], r.dkv_in.at[s], r.dkv_s.at[s], r.dkv_r.at[s], seq=1 - c)

    def own_sequence(ref):
        both = ref[a // buckets].astype(F32)
        picked = both[:, 0, :]
        for bucket in range(1, buckets):
            picked = jnp.where(a % buckets == bucket, both[:, bucket, :], picked)
        return picked

    def first_copy():
        return remote(r.first_out, r.first_in, r.first_s, r.first_r, tensor=near_chip)

    own_place = c * local + t * rows + iota((rows, 1), 0)
    r.first_out[0] = own_sequence(r.inputs).astype(LOW)
    r.first_out[1] = (own_sequence(r.cotangent) * row_mask(own_place)).astype(LOW)
    r.norm_part[...] = jnp.zeros_like(r.norm_part)

    @pl.when(c == 0)
    def _():
        r.kv[:, :, local:total] = jnp.zeros((lines, 2, local, head_width), LOW)


    @pl.when(end_chip)
    def _():
        first_copy().start()

    @pl.when(middle_chip)
    def _():
        first_copy().wait_recv()
        for which in range(2):
            here, beside_it = r.first_out[which].astype(F32), r.first_in[which].astype(F32)
            lower = jnp.where(t % 2 == 0, here, beside_it)
            upper = jnp.where(t % 2 == 0, beside_it, here)
            for j in streams:
                part = slice(j * sub, (j + 1) * sub)
                own_block = jnp.concatenate([lower[part], upper[part]], axis=0)
                if which == 0:
                    r.hidden[j] = own_block
                else:
                    r.upstream[j] = own_block.astype(LOW)

    def on_owner(stage):
        def run(s, j):
            @pl.when(middle_chip)
            def _():
                stage(s, j)

        return run

    def keep_rows(target, s, j, result):
        for half in range(2):
            target[s, half, j * sub : (j + 1) * sub] = result[half * sub : (half + 1) * sub]

    @on_owner
    def enter(s, j):
        xhat, inverse = standard(r.hidden[j])
        r.xhat1[s, j] = xhat
        r.inv1[s, j] = jnp.broadcast_to(inverse, (owned, 128))
        r.nrm[s, j, mine] = (xhat * r.small[s, 0:1] + r.small[s, 1:2]).astype(LOW)
        gather_start(r.nrm, s, 0, j)

    def project(s, j):
        gather_wait(r.nrm, s, 0, j)
        normed = r.nrm[s, j]
        place = row_block(c * STREAMS + j, stream_rows)
        bias_v = r.small[s, 7:8, half_width : half_width + head_width]
        key_rows = dot_nt(normed, r.wq[s, head_width : 2 * head_width])
        value_rows = dot_nt(normed, r.wq[s, 2 * head_width : 3 * head_width]) + bias_v
        r.kv[s, 0, place] = key_rows.astype(LOW)
        r.kv[s, 1, place] = value_rows.astype(LOW)
        gather_sent(r.nrm, s, 0, j)

    def ask(s, j):
        queries = dot_nt(r.nrm[s, j], r.wq[s, 0:head_width]) + r.small[s, 7:8, :head_width]
        r.qry[s, j] = queries.astype(LOW)

    def attend_line(s, j):
        mixed = []
        for head in range(heads):
            cols = head_cols(head)
            times = multiplicity(s, j, head)
            scores = scale * dot_nt(r.qry[s, j, :, cols], r.kv[s, 0, :, cols])
            scores = jnp.where(times > 0.0, scores, MASKED)
            top = jnp.max(scores, axis=-1, keepdims=True)
            terms = times * jnp.exp(scores - top)
            weights = terms / jnp.sum(terms, axis=-1, keepdims=True)
            r.soft[s, j, head] = weights
            mixed.append(dot_nn(weights.astype(LOW), r.kv[s, 1, :, cols]))
        mask = row_mask(place_of(c * local + j * stream_rows + iota((stream_rows, 1), 0)))
        r.mix[s, j] = (jnp.concatenate(mixed, axis=-1) * mask).astype(LOW)

    def leave_attention(s, j):
        scatter_start(s, 0, j, dot_nn(r.mix[s, j], r.wo[s]))

    @on_owner
    def between(s, j):
        middle = r.hidden[j] + scatter_sum(s, 0, j) + r.small[s, 4:5]
        r.middle[j] = middle
        xhat, inverse = standard(middle)
        r.xhat2[s, j] = xhat
        r.inv2[s, j] = jnp.broadcast_to(inverse, (owned, 128))
        r.nmlp[s, j, mine] = (xhat * r.small[s, 2:3] + r.small[s, 3:4]).astype(LOW)
        gather_start(r.nmlp, s, 1, j)

    def feed(s, j):
        gather_wait(r.nmlp, s, 1, j)
        before = dot_nn(r.nmlp[s, j], r.wf[s]) + r.small[s, 6:7, :units]
        bend = jnp.tanh(0.7978845608028654 * (before + 0.044715 * before * before * before))
        r.act[s, j] = (0.5 * before * (1.0 + bend)).astype(LOW)
        r.slope[s, j] = 0.5 * (1.0 + bend) + 0.5 * before * (1.0 - bend * bend) * (
            0.7978845608028654 * (1.0 + 3 * 0.044715 * before * before)
        )

        gather_sent(r.nmlp, s, 1, j)

    def leave_feed(s, j):
        scatter_start(s, 1, j, dot_nn(r.act[s, j], r.wp[s]))

    @on_owner
    def finish(s, j):
        result = r.middle[j] + scatter_sum(s, 1, j) + r.small[s, 5:6]
        keep_rows(r.out_low, s, j, result.astype(LOW))
        r.hidden[j] = result.astype(LOW).astype(F32)

    def small_ready(s):
        @pl.when(a != s)
        def _():
            small_copy(0, a, s).wait_recv()

    small_ready(0)
    for j in streams:
        enter(0, j)

    def forward(s, _):
        need(s, 0)
        for j in streams:
            project(s, j)

        @pl.when(c == 0)
        def _():
            kv_copy(s).start()

        for j in streams:
            ask(s, j)
        rows_start(NRM, s)

        @pl.when(a != s)
        def _():
            count_copy(0, a, s).wait_recv()

        @pl.when(c == 1)
        def _():
            kv_copy(s).wait_recv()

        for j in streams:
            attend_line(s, j)
            if j == 0:
                need(s, 1)
            leave_attention(s, j)
        rows_start(MIX, s)

        @pl.when(s == 0)
        def _():
            pass_later((0, 1), False)

        @pl.when(s > 0)
        def _():
            pass_far(s, 2)
            pass_far(s, 3)

        for j in streams:
            between(s, j)
            scatter_sent(s, 0, j)
        need(s, 2)

        @pl.when(s == 0)
        def _():
            pass_later((2,), False)

        for j in streams:
            feed(s, j)
            if j == 0:
                need(s, 3)
            leave_feed(s, j)

        @pl.when(s == 0)
        def _():
            pass_later((3,), False)

        rows_start(NMLP, s)
        rows_start(ACT, s)

        @pl.when(s + 1 < lines)
        def _():
            small_ready(s + 1)

        for j in streams:
            finish(s, j)
            scatter_sent(s, 1, j)

            @pl.when(s + 1 < lines)
            def _():
                enter(s + 1, j)

        home_start(out_home, s)

        @pl.when(s == 0)
        def _():
            pass_later(range(4), True)

        @pl.when(s + 1 < lines)
        def _():
            pass_far(s + 1, 0)
            pass_far(s + 1, 1)

        return 0

    lax.fori_loop(0, lines, forward, 0)

    @on_owner
    def turn(s, j):
        upstream = r.upstream[j]
        r.ups[s, j, mine] = upstream
        gather_start(r.ups, s, 2, j)
        r.norm_part[s, 5:6] += column_sum(upstream)

    def feed_back(s, j):
        gather_wait(r.ups, s, 2, j)
        grad_pre = (dot_nt(r.ups[s, j], r.wp[s]) * r.slope[s, j]).astype(LOW)
        r.gpre[s, j] = grad_pre
        scatter_start(s, 2, j, dot_nt(grad_pre, r.wf[s]))
        r.norm_part[s, 6:7, :units] += column_sum(grad_pre)
        gather_sent(r.ups, s, 2, j)

    @on_owner
    def between_back(s, j):
        grad = scatter_sum(s, 2, j)
        xhat = r.xhat2[s, j]
        upstream = r.upstream[j].astype(F32)
        grad_middle = upstream + standard_back(
            grad * r.small[s, 2:3], xhat, r.inv2[s, j, :, 0:1]
        )
        r.middle[j] = grad_middle
        branch = grad_middle.astype(LOW)
        r.brn[s, j, mine] = branch
        gather_start(r.brn, s, 3, j)
        r.norm_part[s, 2:3] += column_sum(grad * xhat)
        r.norm_part[s, 3:4] += column_sum(grad)
        r.norm_part[s, 4:5] += column_sum(branch)

    def mixed_back(s, j):
        gather_wait(r.brn, s, 3, j)
        place = place_of(c * local + j * stream_rows + iota((stream_rows, 1), 0))
        r.gmix[j] = (dot_nt(r.brn[s, j], r.wo[s]) * row_mask(place)).astype(LOW)
        gather_sent(r.brn, s, 3, j)

    def attend_line_back(s, j):
        grad_q, grad_k, grad_v = [], [], []
        for head in range(heads):
            cols = head_cols(head)
            weights = r.soft[s, j, head]
            grad_head = r.gmix[j, :, cols]
            grad_weights = dot_nt(grad_head, r.kv[s, 1, :, cols])
            inner = jnp.sum(weights * grad_weights, axis=-1, keepdims=True)
            grad_scores = (weights * (grad_weights - inner)).astype(LOW)
            grad_k.append(scale * dot_tn(grad_scores, r.qry[s, j, :, cols]))
            grad_v.append(dot_tn(weights.astype(LOW), grad_head))
            grad_q.append(scale * dot_nn(grad_scores, r.kv[s, 0, :, cols]))
        for which, grad in enumerate((grad_k, grad_v)):
            grad = jnp.concatenate(grad, axis=-1)
            r.dkv_all[which] = grad if j == 0 else r.dkv_all[which] + grad
        grad_q = jnp.concatenate(grad_q, axis=-1).astype(LOW)
        r.dqkv[s, 0, j] = grad_q
        r.norm_part[s, 7:8, :head_width] += column_sum(grad_q)

    def join_keys(s):
        @pl.when(c == 1)
        def _():
            r.dkv_out[s] = r.dkv_all[:, 0:local].astype(LOW)
            dkv_copy(s).start()

        @pl.when(c == 0)
        def _():
            dkv_copy(s).wait_recv()
            r.dkv_all[:, 0:local] += r.dkv_in[s].astype(F32)

        for which in range(2):
            joined = r.dkv_all[which, my_half].astype(LOW)
            r.dqkv[s, 1 + which] = joined.reshape(r.dqkv.shape[2:])
            if which == 1:
                r.norm_part[s, 7:8, half_width : half_width + head_width] = column_sum(joined)

    def leave_back(s, j):
        product = dot_nn(r.dqkv[s, 0, j], r.wq[s, 0:head_width])
        for which in range(1, 3):
            weight = r.wq[s, which * head_width : (which + 1) * head_width]
            product = product + dot_nn(r.dqkv[s, which, j], weight)
        scatter_start(s, 3, j, product)

    @on_owner
    def finish_back(s, j):
        grad = scatter_sum(s, 3, j)
        xhat = r.xhat1[s, j]
        result = r.middle[j] + standard_back(
            grad * r.small[s, 0:1], xhat, r.inv1[s, j, :, 0:1]
        )
        r.upstream[j] = result.astype(LOW)
        keep_rows(r.grad_low, s, j, result.astype(LOW))
        r.norm_part[s, 0:1] += column_sum(grad * xhat)
        r.norm_part[s, 1:2] += column_sum(grad)

    for j in streams:
        turn(lines - 1, j)

    def backward(index, _):
        s = lines - 1 - index
        for j in streams:
            feed_back(s, j)
        rows_start(UPS, s)
        rows_start(GPRE, s)

        @pl.when(index == 1)
        def _():
            share(ACT)
            share(MIX)

        for j in streams:
            between_back(s, j)
            scatter_sent(s, 2, j)
        for j in streams:
            mixed_back(s, j)
            attend_line_back(s, j)
        join_keys(s)
        rows_start(BRN, s)
        for j in streams:
            leave_back(s, j)
        rows_start(DQKV, s)
        for j in streams:
            finish_back(s, j)
            scatter_sent(s, 3, j)

            @pl.when(s > 0)
            def _():
                turn(s - 1, j)

        norm_start(s)
        home_start(grad_home, s)
        return 0

    lax.fori_loop(0, lines, backward, 0)

    share(GPRE)
    share(DQKV)

    drain(r.norm_all, r.norm_r)
    slot = c * chips + t
    norm_sum = r.norm_all[0]
    for line in range(1, lines):
        norm_sum = norm_sum + r.norm_all[line]
    r.ends[slot] = norm_sum

    def ends_copy(step):
        core, chip = step // chips, step % chips
        view = r.ends.at[slot]
        return remote(
            view,
            view,
            r.ends_s.at[step - 1],
            r.ends_r,
            seq=(c + core) % 2,
            tensor=(t + chip) % chips,
        )

    for step in range(1, 2 * chips):
        ends_copy(step).start()

    for index in range(ACT):
        drain(all_rows[index], r.rows_r.at[index])
    for index in range(ACT, 8):
        share_copy(index, 1 - c).wait_recv()
        share_copy(index, c).wait_send()
    drain(r.acts, r.out_r)
    drain(r.grads, r.grad_r)
    drain(r.ends.at[0 : 2 * chips - 1], r.ends_r)
    for step in range(1, 2 * chips):
        ends_copy(step).wait_send()
    for step in range(1, lines):
        small_copy(step - 1, (a + step) % lines, a).wait_send()
        count_copy(step - 1, (a + step) % lines, a).wait_send()
    for p in range(4):
        for which, line in enumerate((beside(a), above(a))):
            first_hop(p, a, line, which).wait_send()

    @pl.when(end_chip)
    def _():
        first_copy().wait_send()

    def sent(s, _):
        home_sent(out_home, s)
        home_sent(grad_home, s)

        @pl.when(a != s)
        def _():
            norm_copy(s).wait_send()

        @pl.when(c == 0)
        def _():
            kv_copy(s).wait_send()

        @pl.when(c == 1)
        def _():
            dkv_copy(s).wait_send()

        for index in range(8):
            rows_sent(index, s)
        for p in range(4):

            @pl.when((a == beside(s)) | (a == above(s)))
            def _():
                second_hop(p, s, 0).wait_send()

            @pl.when(a != s)
            def _():
                core_hop(p, s, c).wait_send()

        return 0

    lax.fori_loop(0, lines, sent, 0)


def relay_call(inputs, cotangent, lengths, chosen, singles, weights):
    lines = lax.axis_size("section")
    chips = lax.axis_size("tensor")
    rows, buckets, width = inputs.shape[1:]
    local, total, half = rows * chips, 2 * rows * chips, width // 2
    head_width, units = weights["wo_in"].shape[0], weights["wp_in"].shape[0]
    heads = head_width // HDIM
    sub, stream = rows // STREAMS, local // STREAMS
    peers, owned = chips - 1, 2 * sub
    vmem, dma = pltpu.VMEM, pltpu.SemaphoreType.DMA
    operands = dict(
        inputs=inputs,
        cotangent=cotangent,
        lengths=lengths,
        chosen=chosen,
        **singles,
        **weights,
    )

    def space(name):
        if name in weights:
            return pl.ANY
        return pltpu.SMEM if operands[name] is lengths else pltpu.VMEM

    sums = dict(
        acts=((lines, rows, width), LOW),
        grads=((lines, rows, width), LOW),
        ends=((2 * chips, 8, width), F32),
    )
    gathered = dict(
        all_nrm=((lines, 2, STREAMS, stream, half), LOW),
        all_nmlp=((lines, 2, STREAMS, stream, half), LOW),
        all_ups=((lines, 2, STREAMS, stream, half), LOW),
        all_brn=((lines, 2, STREAMS, stream, half), LOW),
        all_act=((lines, 2, STREAMS, stream, units), LOW),
        all_gpre=((lines, 2, STREAMS, stream, units), LOW),
        all_mix=((lines, 2, STREAMS, stream, head_width), LOW),
        all_dqkv=((lines, 2, 3, STREAMS, stream, head_width), LOW),
    )
    outputs = dict(**sums, **gathered)
    scratch = dict(
        wq=vmem((lines,) + weights["wq_in"].shape, LOW),
        wo=vmem((lines,) + weights["wo_in"].shape, LOW),
        wf=vmem((lines,) + weights["wf_in"].shape, LOW),
        wp=vmem((lines,) + weights["wp_in"].shape, LOW),
        small_own=vmem((8, width), F32),
        small=vmem((lines, 8, width), F32),
        count_own=vmem((lines, 8, total), F32),
        count=vmem((lines, 8, total), F32),
        hidden=vmem((STREAMS, owned, width), F32),
        middle=vmem((STREAMS, owned, width), F32),
        upstream=vmem((STREAMS, owned, width), LOW),
        first_out=vmem((2, rows, width), LOW),
        first_in=vmem((2, rows, width), LOW),
        xhat1=vmem((lines, STREAMS, owned, width), F32),
        inv1=vmem((lines, STREAMS, owned, 128), F32),
        xhat2=vmem((lines, STREAMS, owned, width), F32),
        inv2=vmem((lines, STREAMS, owned, 128), F32),
        nrm=vmem((lines, STREAMS, stream, width), LOW),
        nmlp=vmem((lines, STREAMS, stream, width), LOW),
        ups=vmem((lines, STREAMS, stream, width), LOW),
        brn=vmem((lines, STREAMS, stream, width), LOW),
        act=vmem((lines, STREAMS, stream, units), LOW),
        gpre=vmem((lines, STREAMS, stream, units), LOW),
        slope=vmem((lines, STREAMS, stream, units), F32),
        mix=vmem((lines, STREAMS, stream, head_width), LOW),
        qry=vmem((lines, STREAMS, stream, head_width), LOW),
        gmix=vmem((STREAMS, stream, head_width), LOW),
        dqkv=vmem((lines, 3, STREAMS, stream, head_width), LOW),
        kv=vmem((lines, 2, total, head_width), LOW),
        soft=vmem((lines, STREAMS, heads, stream, total), F32),
        near=vmem((STREAMS, stream, total), F32),
        dkv_all=vmem((2, total, head_width), F32),
        dkv_out=vmem((lines, 2, local, head_width), LOW),
        dkv_in=vmem((lines, 2, local, head_width), LOW),
        part=vmem((4, STREAMS, stream, width), LOW),
        arrived=vmem((lines, 4, STREAMS, peers, owned, width), LOW),
        out_low=vmem((lines, 2, rows, width), LOW),
        grad_low=vmem((lines, 2, rows, width), LOW),
        norm_part=vmem((lines, 8, width), F32),
        norm_all=vmem((lines, 8, width), F32),
        w_first_s=dma((4, 2)),
        w_first_r=dma((lines, 4)),
        w_second_s=dma((lines, 4)),
        w_second_r=dma((lines, 4, 2)),
        w_core_s=dma((lines, 4)),
        w_core_r=dma((lines, 4)),
        w_own=dma((4,)),
        small_s=dma((lines - 1,)),
        small_r=dma((lines,)),
        count_s=dma((lines - 1,)),
        count_r=dma((lines,)),
        ag_s=dma((4, STREAMS, peers)),
        ag_r=dma((4, STREAMS, peers)),
        rs_s=dma((4, STREAMS, peers)),
        rs_r=dma((4, STREAMS, peers)),
        kv_s=dma((lines,)),
        kv_r=dma((lines,)),
        dkv_s=dma((lines,)),
        dkv_r=dma((lines,)),
        rows_s=dma((8, lines, 2)),
        rows_r=dma((8,)),
        share_s=dma((4,)),
        share_r=dma((4,)),
        first_s=dma,
        first_r=dma,
        out_s=dma((lines, 2)),
        out_r=dma,
        grad_s=dma((lines, 2)),
        grad_r=dma,
        norm_s=dma((lines,)),
        norm_r=dma,
        ends_s=dma((2 * chips - 1,)),
        ends_r=dma,
    )
    names = tuple(operands) + tuple(outputs) + tuple(scratch)
    results = pl.pallas_call(
        functools.partial(relay_kernel, names),
        out_shape=[jax.ShapeDtypeStruct(shape, kind) for shape, kind in outputs.values()],
        in_specs=[pl.BlockSpec(memory_space=space(name)) for name in operands],
        out_specs=[
            pl.BlockSpec(memory_space=pl.ANY if name in gathered else pltpu.VMEM)
            for name in outputs
        ],
        scratch_shapes=list(scratch.values()),
        compiler_params=pltpu.CompilerParams(
            collective_id=0, has_side_effects=True, vmem_limit_bytes=60 * 2**20
        ),
        name="relay",
    )(*operands.values())
    return dict(zip(outputs, results))


def weights_kernel(names, *refs):
    r = types.SimpleNamespace(**dict(zip(names, refs)))
    step = pl.program_id(0)
    micro_count, rows, buckets, width = r.activations.shape
    chips, units, head_width = r.ends.shape[0] // 2, r.all_act.shape[-1], r.all_mix.shape[-1]

    @pl.when(step == 0)
    def _():
        sums = r.ends[0]
        for other in range(1, 2 * chips):
            sums = sums + r.ends[other]
        singles = (r.ln1_gain, r.ln1_shift, r.ln2_gain, r.ln2_shift, r.b_out, r.b_proj)
        for place, single in enumerate(singles):
            single[...] = sums[place : place + 1]
        for chip in range(chips):
            both = r.ends[chip] + r.ends[chips + chip]
            r.b_fc[:, chip * units : (chip + 1) * units] = both[6:7, :units]
            here = slice(chip * head_width, (chip + 1) * head_width)
            r.b_qv[0:1, here] = both[7:8, :head_width]
            r.b_qv[1:2, here] = both[7:8, width // 2 : width // 2 + head_width]
        for target, source in ((r.activations, r.acts), (r.in_grads, r.grads)):
            for micro in range(micro_count):
                rows_of = [
                    source[micro * buckets + bucket].astype(F32)[:, None, :]
                    for bucket in range(buckets)
                ]
                target[micro] = jnp.concatenate(rows_of, axis=1).astype(LOW)
        for target in (r.w_qkv, r.w_out, r.w_fc, r.w_proj):
            target[...] = jnp.zeros_like(target)

    def rows_of_sequence(ref):
        return ref[0].reshape(2 * chips * rows, ref.shape[-1])

    nrm, nmlp, ups, brn, act, gpre, mix = (
        rows_of_sequence(ref)
        for ref in (r.all_nrm, r.all_nmlp, r.all_ups, r.all_brn, r.all_act, r.all_gpre, r.all_mix)
    )
    r.w_proj[...] += dot_tn(act, ups)
    r.w_fc[...] += dot_tn(nmlp, gpre)
    r.w_out[...] += dot_tn(mix, brn)
    for which in range(3):
        grad = r.all_dqkv[0, :, which].reshape(2 * chips * rows, head_width)
        r.w_qkv[which] += dot_tn(grad, nrm)


def weights_call(relayed, inputs_shape, head_width, units):
    lines = lax.axis_size("section")
    chips = lax.axis_size("tensor")
    width = inputs_shape[-1]
    half = width // 2
    outputs = dict(
        activations=(inputs_shape, LOW),
        in_grads=(inputs_shape, LOW),
        ln1_gain=((1, width), F32),
        ln1_shift=((1, width), F32),
        w_qkv=((3, head_width, half), F32),
        b_qv=((2, width), F32),
        w_out=((head_width, half), F32),
        b_out=((1, width), F32),
        ln2_gain=((1, width), F32),
        ln2_shift=((1, width), F32),
        w_fc=((half, units), F32),
        b_fc=((1, chips * units), F32),
        w_proj=((units, half), F32),
        b_proj=((1, width), F32),
    )

    def spec(array):
        if len(array.shape) < 5:
            return pl.BlockSpec(array.shape, lambda step: (0,) * len(array.shape))
        return pl.BlockSpec(
            (1,) + array.shape[1:], lambda step: (step,) + (0,) * (len(array.shape) - 1)
        )

    def whole(shape):
        return pl.BlockSpec(shape, lambda step: (0,) * len(shape))

    return pl.pallas_call(
        functools.partial(weights_kernel, tuple(relayed) + tuple(outputs)),
        out_shape=[jax.ShapeDtypeStruct(shape, kind) for shape, kind in outputs.values()],
        grid=(lines,),
        in_specs=[spec(array) for array in relayed.values()],
        out_specs=[whole(shape) for shape, _ in outputs.values()],
        compiler_params=pltpu.CompilerParams(vmem_limit_bytes=60 * 2**20),
        name="weight_gradients",
    )(*relayed.values())


def on_line(
    inputs,
    cotangent,
    lengths,
    chosen,
    ln1_gain,
    ln1_shift,
    w_qkv,
    b_qv,
    w_out,
    b_out,
    ln2_gain,
    ln2_shift,
    w_fc,
    b_fc,
    w_proj,
    b_proj,
):
    head_width, units = w_out.shape[1], w_fc.shape[2]
    singles = dict(
        ln1_gain=ln1_gain,
        ln1_shift=ln1_shift,
        ln2_gain=ln2_gain,
        ln2_shift=ln2_shift,
        b_out=b_out,
        b_proj=b_proj,
        b_fc=b_fc,
        b_qv=b_qv[0],
    )
    weights = dict(
        wq_in=jnp.swapaxes(w_qkv[0], 1, 2).reshape(-1, inputs.shape[-1]),
        wo_in=w_out[0],
        wf_in=w_fc[0],
        wp_in=w_proj[0],
    )
    picks = chosen.reshape((-1,) + chosen.shape[-2:])
    relayed = relay_call(inputs, cotangent, lengths, picks, singles, weights)
    results = list(weights_call(relayed, inputs.shape, head_width, units))
    results[4] = jnp.swapaxes(results[4], 1, 2)
    vectors = (2, 3, 7, 8, 9, 11, 13)
    return tuple(
        result if place in vectors else result[None] for place, result in enumerate(results)
    )


def fits_lines(mesh):
    return mesh.shape["section"] == 4 and mesh.shape["seq"] == 2 and mesh.shape["tensor"] == 4


def solution(mesh):
    placed = (
        P(None, ("seq", "tensor"), None, None),
        P(None, ("seq", "tensor"), None, None),
        P(),
        P("section", None, None, "tensor", "seq", None),
        P("section", None),
        P("section", None),
        P("section", None, None, "tensor"),
        P("section", None, "tensor"),
        P("section", "tensor", None),
        P("section", None),
        P("section", None),
        P("section", None),
        P("section", None, "tensor"),
        P("section", "tensor"),
        P("section", "tensor", None),
        P("section", None),
    )
    return jax.shard_map(
        on_line if fits_lines(mesh) else on_device,
        mesh=mesh,
        in_specs=placed,
        out_specs=(
            P("section", None, ("seq", "tensor"), None, None),
            P("section", None, ("seq", "tensor"), None, None),
            P("section", None),
            P("section", None),
            P("section", None, "seq", "tensor"),
            P("section", None, None),
            P("section", "tensor", "seq"),
            P("section", None),
            P("section", None),
            P("section", None),
            P("section", "seq", "tensor"),
            P("section", None),
            P("section", "tensor", "seq"),
            P("section", None),
        ),
        check_vma=False,
    )
```

```python
import functools
import types

import jax
import jax.numpy as jnp
from jax import lax
from jax.experimental import pallas as pl
from jax.experimental.pallas import tpu as pltpu
from jax.sharding import PartitionSpec as P

HDIM = 64
WIN = 64
QB = 64
KSEL = 64


NORM_EPS = 1e-05
MASKED = -1000000000.0


def from_behind(value, axis, steps):
    count = lax.axis_size(axis)
    first, last = (max(0, -steps), min(count, count - steps))
    return lax.ppermute(value, axis, [(source, source + steps) for source in range(first, last)])


def layer_norm(values, gain, shift):
    average = jnp.mean(values, axis=-1, keepdims=True)
    centred = values - average
    variance = jnp.mean(centred * centred, axis=-1, keepdims=True)
    return centred * lax.rsqrt(variance + NORM_EPS) * gain + shift


def gelu_tanh(values):
    return (
        0.5
        * values
        * (1.0 + jnp.tanh(0.7978845608028654 * (values + 0.044715 * values * values * values)))
    )


def gather_rows(row_block):
    return lax.all_gather(row_block, "tensor", axis=0, tiled=True)


def scatter_product(left_rows, weight, formula):
    return lax.psum_scatter(
        jnp.einsum(formula, left_rows, weight, preferred_element_type=jnp.float32).astype(
            jnp.bfloat16
        ),
        "tensor",
        scatter_dimension=0,
        tiled=True,
    ).astype(jnp.float32)


def near_slabs(full_rows, seq_start, seq_first, length_local):
    buckets = full_rows.shape[1]
    heads_local = full_rows.shape[2] // HDIM
    blocks = length_local // QB
    earlier = lax.dynamic_slice_in_dim(full_rows, jnp.maximum(seq_start - WIN, 0), WIN, 0)
    earlier = jnp.where(seq_first, jnp.zeros_like(earlier), earlier)
    local_part = lax.dynamic_slice_in_dim(full_rows, seq_start, length_local, 0)
    segment = jnp.concatenate([earlier, local_part], 0).reshape(
        length_local + WIN, buckets, heads_local, HDIM
    )
    return jnp.concatenate(
        [
            segment[offset_index * QB : offset_index * QB + length_local].reshape(
                blocks, QB, buckets, heads_local, HDIM
            )
            for offset_index in range(WIN // QB + 1)
        ],
        1,
    )


def far_rows(full_rows, flat_index):
    total_rows, buckets, feature_width = full_rows.shape
    heads_local = feature_width // HDIM
    return jnp.take(full_rows.reshape(total_rows * buckets * heads_local, HDIM), flat_index, axis=0)


def key_geometry(chosen_now, seq_start, blocks):
    buckets, heads_local = (chosen_now.shape[0], chosen_now.shape[1])
    bucket_ids = lax.broadcasted_iota(jnp.int32, chosen_now.shape, 0)
    head_ids = lax.broadcasted_iota(jnp.int32, chosen_now.shape, 1)
    flat_index = (chosen_now * buckets + bucket_ids) * heads_local + head_ids
    block_start = seq_start + QB * lax.broadcasted_iota(jnp.int32, (blocks, 1, 1), 0)
    query_ids = lax.broadcasted_iota(jnp.int32, (1, QB, 1), 1)
    key_ids = lax.broadcasted_iota(jnp.int32, (1, 1, WIN + QB), 2)
    distance = query_ids + WIN - key_ids
    near_ok = (distance >= 0) & (distance < WIN) & (block_start + key_ids - WIN >= 0)
    far_ok = chosen_now + WIN <= block_start.reshape(1, 1, blocks, 1)
    near_mask = jnp.broadcast_to(
        near_ok[:, None, None], (blocks, buckets, heads_local, QB, WIN + QB)
    )
    far_mask = jnp.broadcast_to(
        jnp.transpose(far_ok, (2, 0, 1, 3))[:, :, :, None, :],
        (blocks, buckets, heads_local, QB, KSEL),
    )
    return (flat_index, jnp.concatenate([near_mask, far_mask], -1))


def attention_setup(queries, key_rows, value_rows, chosen_now, seq_start, seq_first):
    length_local, buckets, feature_width = queries.shape
    heads_local = feature_width // HDIM
    blocks = length_local // QB
    query_blocks = queries.reshape(blocks, QB, buckets, heads_local, HDIM)
    flat_index, key_mask = key_geometry(chosen_now, seq_start, blocks)
    near_keys = near_slabs(key_rows, seq_start, seq_first, length_local)
    near_values = near_slabs(value_rows, seq_start, seq_first, length_local)
    far_keys = far_rows(key_rows, flat_index)
    far_values = far_rows(value_rows, flat_index)
    near_scores = jnp.einsum(
        "bqnhe,btnhe->bnhqt", query_blocks, near_keys, preferred_element_type=jnp.float32
    )
    far_scores = jnp.einsum(
        "bqnhe,nhbke->bnhqk", query_blocks, far_keys, preferred_element_type=jnp.float32
    )
    scores = jnp.where(
        key_mask, HDIM ** (-0.5) * jnp.concatenate([near_scores, far_scores], -1), MASKED
    )
    return (query_blocks, near_keys, near_values, far_keys, far_values, flat_index, scores)


def attend(queries, key_rows, value_rows, chosen_now, seq_start, seq_first):
    query_blocks, near_keys, near_values, far_keys, far_values, flat_index, scores = (
        attention_setup(queries, key_rows, value_rows, chosen_now, seq_start, seq_first)
    )
    span = WIN + QB
    row_top = jnp.max(scores, -1, keepdims=True)
    exp_terms = jnp.exp(scores - row_top)
    row_total = jnp.sum(exp_terms, -1, keepdims=True)
    softmax_low = (exp_terms / row_total).astype(jnp.bfloat16)
    near_part = jnp.einsum(
        "bnhqt,btnhe->bqnhe",
        softmax_low[..., :span],
        near_values,
        preferred_element_type=jnp.float32,
    )
    far_part = jnp.einsum(
        "bnhqk,nhbke->bqnhe",
        softmax_low[..., span:],
        far_values,
        preferred_element_type=jnp.float32,
    )
    return ((near_part + far_part).reshape(queries.shape), row_top + jnp.log(row_total))


def spread_back(near_grad, far_grad, flat_index, seq_start, seq_first, total_rows):
    blocks, span, buckets, heads_local, head_size = near_grad.shape
    length_local = blocks * QB
    feature_width = heads_local * head_size
    segment = jnp.zeros((length_local + WIN, buckets, heads_local, head_size), jnp.float32)
    for offset_index in range(WIN // QB + 1):
        piece = near_grad[:, offset_index * QB : (offset_index + 1) * QB].reshape(
            length_local, buckets, heads_local, head_size
        )
        segment = segment.at[offset_index * QB : offset_index * QB + length_local].add(piece)
    full_rows = jnp.zeros((total_rows * buckets * heads_local, head_size), jnp.float32)
    full_rows = full_rows.at[flat_index.reshape(-1)].add(far_grad.reshape(-1, head_size))
    full_rows = full_rows.reshape(total_rows, buckets, feature_width)
    local_part = segment[WIN:].reshape(length_local, buckets, feature_width)
    earlier = jnp.where(seq_first, 0.0, segment[:WIN].reshape(WIN, buckets, feature_width))
    full_rows = lax.dynamic_update_slice_in_dim(
        full_rows,
        lax.dynamic_slice_in_dim(full_rows, seq_start, length_local, 0) + local_part,
        seq_start,
        0,
    )
    earlier_start = jnp.maximum(seq_start - WIN, 0)
    full_rows = lax.dynamic_update_slice_in_dim(
        full_rows,
        lax.dynamic_slice_in_dim(full_rows, earlier_start, WIN, 0) + earlier,
        earlier_start,
        0,
    )
    return full_rows


def attend_back(
    queries, key_rows, value_rows, chosen_now, seq_start, seq_first, log_total, grad_mixed
):
    query_blocks, near_keys, near_values, far_keys, far_values, flat_index, scores = (
        attention_setup(queries, key_rows, value_rows, chosen_now, seq_start, seq_first)
    )
    span = WIN + QB
    score_scale = HDIM ** (-0.5)
    grad_blocks = grad_mixed.reshape(query_blocks.shape)
    weights_full = jnp.exp(scores - log_total)
    softmax_low = weights_full.astype(jnp.bfloat16)
    grad_near_weights = jnp.einsum(
        "bqnhe,btnhe->bnhqt", grad_blocks, near_values, preferred_element_type=jnp.float32
    )
    grad_far_weights = jnp.einsum(
        "bqnhe,nhbke->bnhqk", grad_blocks, far_values, preferred_element_type=jnp.float32
    )
    grad_weights = jnp.concatenate([grad_near_weights, grad_far_weights], -1)
    row_dot = jnp.sum(weights_full * grad_weights, -1, keepdims=True)
    grad_scores = (weights_full * (grad_weights - row_dot)).astype(jnp.bfloat16)
    grad_near, grad_far = (grad_scores[..., :span], grad_scores[..., span:])
    grad_queries = score_scale * (
        jnp.einsum("bnhqt,btnhe->bqnhe", grad_near, near_keys, preferred_element_type=jnp.float32)
        + jnp.einsum("bnhqk,nhbke->bqnhe", grad_far, far_keys, preferred_element_type=jnp.float32)
    )
    near_key_grad = score_scale * jnp.einsum(
        "bnhqt,bqnhe->btnhe", grad_near, query_blocks, preferred_element_type=jnp.float32
    )
    far_key_grad = score_scale * jnp.einsum(
        "bnhqk,bqnhe->nhbke", grad_far, query_blocks, preferred_element_type=jnp.float32
    )
    near_value_grad = jnp.einsum(
        "bnhqt,bqnhe->btnhe",
        softmax_low[..., :span],
        grad_blocks,
        preferred_element_type=jnp.float32,
    )
    far_value_grad = jnp.einsum(
        "bnhqk,bqnhe->nhbke",
        softmax_low[..., span:],
        grad_blocks,
        preferred_element_type=jnp.float32,
    )
    total_rows = key_rows.shape[0]
    key_grad = spread_back(
        near_key_grad, far_key_grad, flat_index, seq_start, seq_first, total_rows
    )
    value_grad = spread_back(
        near_value_grad, far_value_grad, flat_index, seq_start, seq_first, total_rows
    )
    return (grad_queries.reshape(queries.shape), key_grad, value_grad)


def forward_pass(hidden, params, chosen_now, query_mask, seq_start, seq_first, finish):
    (
        ln1_gain,
        ln1_shift,
        w_qkv,
        b_qv,
        w_out,
        b_out,
        ln2_gain,
        ln2_shift,
        w_fc,
        b_fc,
        w_proj,
        b_proj,
    ) = params
    hidden_wide = hidden.astype(jnp.float32)
    normed_all = gather_rows(layer_norm(hidden_wide, ln1_gain, ln1_shift).astype(jnp.bfloat16))
    projected = jnp.einsum("pnd,jdc->jpnc", normed_all, w_qkv, preferred_element_type=jnp.float32)
    queries = (projected[0] + b_qv[0]).astype(jnp.bfloat16)
    key_rows, value_rows = (
        lax.all_gather(projected[1].astype(jnp.bfloat16), "seq", axis=0, tiled=True),
        lax.all_gather((projected[2] + b_qv[1]).astype(jnp.bfloat16), "seq", axis=0, tiled=True),
    )
    attended, log_total = attend(queries, key_rows, value_rows, chosen_now, seq_start, seq_first)
    mixed_rows = (attended * query_mask[:, :, None]).astype(jnp.bfloat16)
    middle = hidden_wide + scatter_product(mixed_rows, w_out, "pnc,cd->pnd") + b_out
    normed_mlp = gather_rows(layer_norm(middle, ln2_gain, ln2_shift).astype(jnp.bfloat16))
    pre_active = (
        jnp.einsum("pnd,df->pnf", normed_mlp, w_fc, preferred_element_type=jnp.float32) + b_fc
    )
    active = gelu_tanh(pre_active).astype(jnp.bfloat16)
    if not finish:
        return (
            normed_all,
            queries,
            key_rows,
            value_rows,
            log_total,
            mixed_rows,
            middle,
            normed_mlp,
            pre_active,
            active,
        )
    output = (middle + scatter_product(active, w_proj, "pnf,fd->pnd") + b_proj).astype(jnp.bfloat16)
    return (output, (key_rows, value_rows))


def backward_pass(hidden, upstream, params, chosen_now, query_mask, seq_start, seq_first):
    (
        ln1_gain,
        ln1_shift,
        w_qkv,
        b_qv,
        w_out,
        b_out,
        ln2_gain,
        ln2_shift,
        w_fc,
        b_fc,
        w_proj,
        b_proj,
    ) = params
    (
        normed_all,
        queries,
        key_rows,
        value_rows,
        log_total,
        mixed_rows,
        middle,
        normed_mlp,
        pre_active,
        active,
    ) = forward_pass(hidden, params, chosen_now, query_mask, seq_start, seq_first, False)
    upstream_all = gather_rows(upstream)
    grad_w_proj = jnp.einsum(
        "pnf,pnd->fd", active, upstream_all, preferred_element_type=jnp.float32
    )
    grad_b_proj = jnp.sum(upstream.astype(jnp.float32), axis=(0, 1))
    grad_active = jnp.einsum(
        "pnd,fd->pnf", upstream_all, w_proj, preferred_element_type=jnp.float32
    )
    unused_value, gelu_pull = jax.vjp(gelu_tanh, pre_active)
    grad_pre = gelu_pull(grad_active)[0].astype(jnp.bfloat16)
    grad_w_fc = jnp.einsum("pnd,pnf->df", normed_mlp, grad_pre, preferred_element_type=jnp.float32)
    grad_b_fc = jnp.sum(grad_pre.astype(jnp.float32), axis=(0, 1))
    grad_normed_mlp = scatter_product(grad_pre, w_fc, "pnf,df->pnd")
    unused_norm, second_pull = jax.vjp(layer_norm, middle, ln2_gain, ln2_shift)
    grad_mid_norm, grad_ln2_gain, grad_ln2_shift = second_pull(grad_normed_mlp)
    grad_middle = upstream.astype(jnp.float32) + grad_mid_norm
    grad_branch = grad_middle.astype(jnp.bfloat16)
    grad_b_out = jnp.sum(grad_branch.astype(jnp.float32), axis=(0, 1))
    branch_all = gather_rows(grad_branch)
    grad_w_out = jnp.einsum(
        "pnc,pnd->cd", mixed_rows, branch_all, preferred_element_type=jnp.float32
    )
    grad_mixed = jnp.einsum(
        "pnd,cd->pnc", branch_all, w_out, preferred_element_type=jnp.float32
    ).astype(jnp.bfloat16) * query_mask[:, :, None].astype(jnp.bfloat16)
    grad_queries, key_grad_all, value_grad_all = attend_back(
        queries, key_rows, value_rows, chosen_now, seq_start, seq_first, log_total, grad_mixed
    )
    key_grad, value_grad = (
        lax.psum_scatter(
            key_grad_all.astype(jnp.bfloat16), "seq", scatter_dimension=0, tiled=True
        ).astype(jnp.float32),
        lax.psum_scatter(
            value_grad_all.astype(jnp.bfloat16), "seq", scatter_dimension=0, tiled=True
        ).astype(jnp.float32),
    )
    grad_project = jnp.stack(
        [
            grad_queries.astype(jnp.bfloat16),
            key_grad.astype(jnp.bfloat16),
            value_grad.astype(jnp.bfloat16),
        ],
        2,
    )
    grad_w_qkv = jnp.einsum(
        "pnd,pnjc->jdc", normed_all, grad_project, preferred_element_type=jnp.float32
    )
    grad_b_qv = jnp.sum(grad_project[:, :, 0::2].astype(jnp.float32), axis=(0, 1))
    grad_normed = scatter_product(grad_project, w_qkv, "pnjc,jdc->pnd")
    unused_first, first_pull = jax.vjp(layer_norm, hidden.astype(jnp.float32), ln1_gain, ln1_shift)
    grad_in_norm, grad_ln1_gain, grad_ln1_shift = first_pull(grad_normed)
    grad_hidden = (grad_middle + grad_in_norm).astype(jnp.bfloat16)
    block_grads = (
        grad_ln1_gain,
        grad_ln1_shift,
        grad_w_qkv,
        grad_b_qv,
        grad_w_out,
        grad_b_out,
        grad_ln2_gain,
        grad_ln2_shift,
        grad_w_fc,
        grad_b_fc,
        grad_w_proj,
        grad_b_proj,
    )
    return (grad_hidden, block_grads)


def on_device(
    inputs,
    cotangent,
    lengths,
    chosen,
    ln1_gain,
    ln1_shift,
    w_qkv,
    b_qv,
    w_out,
    b_out,
    ln2_gain,
    ln2_shift,
    w_fc,
    b_fc,
    w_proj,
    b_proj,
):
    params = tuple(
        (
            weight_array[0]
            for weight_array in (
                ln1_gain,
                ln1_shift,
                w_qkv,
                b_qv,
                w_out,
                b_out,
                ln2_gain,
                ln2_shift,
                w_fc,
                b_fc,
                w_proj,
                b_proj,
            )
        )
    )
    section_index = lax.axis_index("section")
    section_count = lax.axis_size("section")
    seq_index = lax.axis_index("seq")
    tensor_index = lax.axis_index("tensor")
    tensor_count = lax.axis_size("tensor")
    micro_count, rows_local, buckets, feature_width = inputs.shape
    length_local = rows_local * tensor_count
    heads_width = w_qkv.shape[-1]
    seq_start = seq_index * length_local
    seq_first = seq_index == 0
    positions = seq_start + lax.broadcasted_iota(jnp.int32, (micro_count, length_local, buckets), 1)
    mask_all = (positions < lengths[:, None, :]).astype(jnp.float32)
    mask_rows = lax.dynamic_slice_in_dim(mask_all, tensor_index * rows_local, rows_local, 1)
    step_count = micro_count + section_count - 1
    chosen_section = chosen[0]
    received = jnp.zeros((rows_local, buckets, feature_width), jnp.bfloat16)
    stored = jnp.zeros((micro_count, rows_local, buckets, feature_width), jnp.bfloat16)
    outputs = jnp.zeros_like(stored)
    for step_index in range(step_count):
        micro_index = step_index - section_index
        running = (micro_index >= 0) & (micro_index < micro_count)
        slot_index = jnp.clip(micro_index, 0, micro_count - 1)
        block_in = jnp.where(
            section_index == 0, lax.dynamic_index_in_dim(inputs, slot_index, 0, False), received
        )
        chosen_now = lax.dynamic_index_in_dim(chosen_section, slot_index, 0, False)
        query_mask = lax.dynamic_index_in_dim(mask_all, slot_index, 0, False)
        result, key_pair = forward_pass(
            block_in, params, chosen_now, query_mask, seq_start, seq_first, True
        )
        stored = jnp.where(
            running, lax.dynamic_update_index_in_dim(stored, block_in, slot_index, 0), stored
        )
        outputs = jnp.where(
            running, lax.dynamic_update_index_in_dim(outputs, result, slot_index, 0), outputs
        )
        received = from_behind(result, "section", 1)
    back_received = jnp.zeros((rows_local, buckets, feature_width), jnp.bfloat16)
    in_grads = jnp.zeros_like(stored)
    totals = None
    for step_index in range(step_count):
        micro_index = step_index - (section_count - 1 - section_index)
        running = (micro_index >= 0) & (micro_index < micro_count)
        slot_index = jnp.clip(micro_index, 0, micro_count - 1)
        chosen_now = lax.dynamic_index_in_dim(chosen_section, slot_index, 0, False)
        query_mask = lax.dynamic_index_in_dim(mask_all, slot_index, 0, False)
        local_mask = lax.dynamic_index_in_dim(mask_rows, slot_index, 0, False)
        top_grad = (
            lax.dynamic_index_in_dim(cotangent, slot_index, 0, False).astype(jnp.float32)
            * local_mask[:, :, None]
        ).astype(jnp.bfloat16)
        upstream = jnp.where(section_index == section_count - 1, top_grad, back_received)
        hidden = lax.dynamic_index_in_dim(stored, slot_index, 0, False)
        grad_hidden, block_grads = backward_pass(
            hidden, upstream, params, chosen_now, query_mask, seq_start, seq_first
        )
        block_grads = tuple(
            (jnp.where(running, grad_part, jnp.zeros_like(grad_part)) for grad_part in block_grads)
        )
        totals = (
            block_grads
            if step_index == 0
            else tuple(
                (total_part + grad_part for total_part, grad_part in zip(totals, block_grads))
            )
        )
        in_grads = jnp.where(
            running, lax.dynamic_update_index_in_dim(in_grads, grad_hidden, slot_index, 0), in_grads
        )
        back_received = from_behind(grad_hidden, "section", -1)
    (
        sum_ln1_gain,
        sum_ln1_shift,
        sum_w_qkv,
        sum_b_qv,
        sum_w_out,
        sum_b_out,
        sum_ln2_gain,
        sum_ln2_shift,
        sum_w_fc,
        sum_b_fc,
        sum_w_proj,
        sum_b_proj,
    ) = totals
    part_qkv, part_out, part_fc, part_proj = (
        lax.psum_scatter(
            sum_w_qkv.astype(jnp.bfloat16), "seq", scatter_dimension=1, tiled=True
        ).astype(jnp.float32),
        lax.psum_scatter(
            sum_w_out.astype(jnp.bfloat16), "seq", scatter_dimension=1, tiled=True
        ).astype(jnp.float32),
        lax.psum_scatter(
            sum_w_fc.astype(jnp.bfloat16), "seq", scatter_dimension=0, tiled=True
        ).astype(jnp.float32),
        lax.psum_scatter(
            sum_w_proj.astype(jnp.bfloat16), "seq", scatter_dimension=1, tiled=True
        ).astype(jnp.float32),
    )
    bias_qv = lax.dynamic_update_slice_in_dim(
        jnp.zeros((2, feature_width), jnp.float32), sum_b_qv, tensor_index * heads_width, 1
    )
    units_local = sum_b_fc.shape[0]
    bias_fc = lax.dynamic_update_slice_in_dim(
        jnp.zeros((units_local * tensor_count,), jnp.float32),
        sum_b_fc,
        tensor_index * units_local,
        0,
    )
    small_sums = lax.psum(
        (
            sum_ln1_gain,
            sum_ln1_shift,
            bias_qv,
            sum_b_out,
            sum_ln2_gain,
            sum_ln2_shift,
            bias_fc,
            sum_b_proj,
        ),
        ("seq", "tensor"),
    )
    return (
        outputs[None],
        in_grads[None],
        small_sums[0][None],
        small_sums[1][None],
        part_qkv[None],
        small_sums[2][None],
        part_out[None],
        small_sums[3][None],
        small_sums[4][None],
        small_sums[5][None],
        part_fc[None],
        small_sums[6][None],
        part_proj[None],
        small_sums[7][None],
    )


STREAMS = 4
NRM, NMLP, UPS, BRN, ACT, GPRE, MIX, DQKV = range(8)
F32 = jnp.float32
LOW = jnp.bfloat16
MESH_ID = pl.DeviceIdType.MESH


def dot_nn(left, right):
    return lax.dot_general(left, right, (((1,), (0,)), ((), ())), preferred_element_type=F32)


def dot_nt(left, right):
    return lax.dot_general(left, right, (((1,), (1,)), ((), ())), preferred_element_type=F32)


def dot_tn(left, right):
    return lax.dot_general(left, right, (((0,), (0,)), ((), ())), preferred_element_type=F32)


def standard(rows):
    centred = rows - jnp.mean(rows, axis=-1, keepdims=True)
    scale = lax.rsqrt(jnp.mean(centred * centred, axis=-1, keepdims=True) + NORM_EPS)
    return centred * scale, scale


def standard_back(grad, xhat, scale):
    inner = jnp.mean(grad * xhat, axis=-1, keepdims=True)
    return scale * (grad - jnp.mean(grad, axis=-1, keepdims=True) - xhat * inner)


def column_sum(rows):
    return jnp.sum(rows.astype(F32), axis=0, keepdims=True)


def relay_kernel(names, *refs):
    r = types.SimpleNamespace(**dict(zip(names, refs)))
    a, c, t = (lax.axis_index(name) for name in ("section", "seq", "tensor"))
    lines = lax.axis_size("section")
    chips = lax.axis_size("tensor")
    rows, buckets, width = r.inputs.shape[1:]
    half_width = width // 2
    local = rows * chips
    total = 2 * local
    stream_rows = local // STREAMS
    head_width = r.wo_in.shape[0]
    heads = head_width // HDIM
    blocks = local // QB
    units = r.wp_in.shape[0]
    scale = HDIM ** (-0.5)
    streams = range(STREAMS)

    def remote(src, dst, send, recv, **target):
        return pltpu.make_async_remote_copy(
            src_ref=src,
            dst_ref=dst,
            send_sem=send,
            recv_sem=recv,
            device_id=target,
            device_id_type=MESH_ID,
        )

    def drain(ref, sem):
        pltpu.make_async_copy(ref, ref, sem).wait()

    def row_block(index, size):
        return pl.ds(pl.multiple_of(index * size, size), size)

    near_chip = t + 1 - 2 * (t % 2)
    over_chip = (t + 2) % 4
    across_chip = 3 - t
    middle_chip = (t == 1) | (t == 2)
    end_chip = (t == 0) | (t == 3)
    owned = stream_rows // 2
    mine = row_block(t - 1, owned)
    my_half = row_block(c, local)

    barrier = pltpu.get_barrier_semaphore()
    for core in range(2):
        for step in range(1, chips):
            there = {"tensor": (t + step) % chips, "seq": core}
            pl.semaphore_signal(barrier, inc=1, device_id=there, device_id_type=MESH_ID)
        for step in range(1, lines):
            there = {"section": (a + step) % lines, "seq": core}
            pl.semaphore_signal(barrier, inc=1, device_id=there, device_id_type=MESH_ID)
    for step in range(1, lines):
        there = {"section": (a + step) % lines, "tensor": near_chip}
        pl.semaphore_signal(barrier, inc=1, device_id=there, device_id_type=MESH_ID)
    pl.semaphore_signal(barrier, inc=1, device_id={"seq": 1 - c}, device_id_type=MESH_ID)
    pl.semaphore_wait(barrier, 2 * (chips - 1) + 3 * (lines - 1) + 1)

    def beside(s):
        return s + 1 - 2 * (s % 2)

    def above(s):
        return (s + 2) % 4

    def store(p):
        return (r.wq, r.wo, r.wf, r.wp)[p]

    def source(p):
        return (r.wq_in, r.wo_in, r.wf_in, r.wp_in)[p]

    def height(p):
        return source(p).shape[0]

    def core_half(p, s, core):
        return store(p).at[s, row_block(core, height(p) // 2)]

    def first_hop(p, s, neighbour, which):
        return remote(
            source(p).at[row_block(c, height(p) // 2)],
            core_half(p, s, c),
            r.w_first_s.at[p, which],
            r.w_first_r.at[s, p],
            section=neighbour,
        )

    def second_hop(p, s, which):
        view = store(p).at[s, row_block(2 * c + which, height(p) // 4)]
        return remote(
            view, view, r.w_second_s.at[s, p], r.w_second_r.at[s, p, which], section=3 - s
        )

    def core_hop(p, s, core):
        view = core_half(p, s, core)
        return remote(view, view, r.w_core_s.at[s, p], r.w_core_r.at[s, p], seq=1 - c)

    def own_copy(p):
        return pltpu.make_async_copy(source(p), store(p).at[a], r.w_own.at[p])

    def pass_on(s, p, which):
        line = (beside(s), above(s))[which]

        @pl.when(a == line)
        def _():
            first_hop(p, s, line, which).wait_recv()
            second_hop(p, s, which).start()
            core_hop(p, s, c).start()

    def pass_later(pieces, at_first):
        for later in range(1, lines):
            for which in range(2):
                if ((beside(later), above(later))[which] == 0) == at_first:
                    for p in pieces:
                        pass_on(later, p, which)

    def pass_far(s, p):
        @pl.when(a == 3 - s)
        def _():
            second_hop(p, s, 0).wait_recv()
            second_hop(p, s, 1).wait_recv()
            core_hop(p, s, c).start()

    def need(s, p):
        @pl.when(s == 0)
        def _():
            pass_on(0, p, 0)
            pass_on(0, p, 1)
            pass_far(0, p)

        @pl.when(a == s)
        def _():
            own_copy(p).wait()

        @pl.when(a != s)
        def _():
            core_hop(p, s, 1 - c).wait_recv()

    def small_copy(step, line, slot):
        return remote(
            r.small_own, r.small.at[slot], r.small_s.at[step], r.small_r.at[slot], section=line
        )

    def count_copy(step, line, slot):
        return remote(
            r.count_own.at[line],
            r.count.at[slot],
            r.count_s.at[step],
            r.count_r.at[slot],
            section=line,
        )

    singles = (r.ln1_gain, r.ln1_shift, r.ln2_gain, r.ln2_shift, r.b_out, r.b_proj)
    for place, single in enumerate(singles):
        r.small_own[place : place + 1] = single[...]
    r.small_own[6:7, :units] = r.b_fc[...]
    r.small_own[7:8, :head_width] = r.b_qv[0:1]
    r.small_own[7:8, half_width : half_width + head_width] = r.b_qv[1:2]
    for step in range(1, lines):
        small_copy(step - 1, (a + step) % lines, a).start()
    for p in range(4):
        for which, line in enumerate((beside(a), above(a))):
            first_hop(p, a, line, which).start()
    for p in range(4):
        own_copy(p).start()
    r.small[a] = r.small_own[...]

    def place_of(index):
        inside = index % local
        stream, left = inside // stream_rows, inside % stream_rows
        first = (index // local) * local + (left // owned) * (local // 2)
        return first + stream * owned + left % owned

    def iota(shape, dimension):
        return lax.broadcasted_iota(jnp.int32, shape, dimension)

    square = jnp.where(iota((KSEL, KSEL), 0) == iota((KSEL, KSEL), 1), 1.0, 0.0).astype(LOW)
    position = place_of(iota((KSEL, total), 1)).astype(F32)
    for pair in range(lines * heads):
        line, head = pair // heads, pair % heads
        columns = dot_nt(square, r.chosen[pair].astype(F32).astype(LOW))
        for block in range(blocks):
            pick = head * blocks + block
            r.count_own[line, pick : pick + 1, :] = jnp.sum(
                jnp.where(columns[:, block : block + 1] == position, 1.0, 0.0),
                axis=0,
                keepdims=True,
            )
    for step in range(1, lines):
        count_copy(step - 1, (a + step) % lines, a).start()
    r.count[a] = r.count_own[a]

    NEAR, OVER, ACROSS = range(3)

    def gather(buffer, s, kind, j, owner, target, slot):
        view = buffer.at[s, j, row_block(owner - 1, owned)]
        return remote(
            view, view, r.ag_s.at[kind, j, slot], r.ag_r.at[kind, j, slot], tensor=target
        )

    def gather_start(buffer, s, kind, j):
        gather(buffer, s, kind, j, t, over_chip, OVER).start()
        gather(buffer, s, kind, j, t, across_chip, ACROSS).start()
        gather(buffer, s, kind, j, t, near_chip, NEAR).start()

    def gather_wait(buffer, s, kind, j):
        @pl.when(middle_chip)
        def _():
            gather(buffer, s, kind, j, across_chip, across_chip, ACROSS).wait_recv()

        @pl.when(end_chip)
        def _():
            gather(buffer, s, kind, j, near_chip, near_chip, NEAR).wait_recv()
            gather(buffer, s, kind, j, over_chip, over_chip, OVER).wait_recv()

    def gather_sent(buffer, s, kind, j):
        @pl.when(middle_chip)
        def _():
            gather(buffer, s, kind, j, t, over_chip, OVER).wait_send()
            gather(buffer, s, kind, j, t, across_chip, ACROSS).wait_send()
            gather(buffer, s, kind, j, t, near_chip, NEAR).wait_send()

    def scatter(s, kind, j, owner, slot):
        return remote(
            r.part.at[kind, j, row_block(owner - 1, owned)],
            r.arrived.at[s, kind, j, slot],
            r.rs_s.at[kind, j, slot],
            r.rs_r.at[kind, j, slot],
            tensor=owner,
        )

    def scatter_start(s, kind, j, product):
        r.part[kind, j] = product.astype(LOW)

        @pl.when(end_chip)
        def _():
            scatter(s, kind, j, over_chip, OVER).start()
            scatter(s, kind, j, near_chip, NEAR).start()

        @pl.when(middle_chip)
        def _():
            scatter(s, kind, j, across_chip, ACROSS).start()

    def scatter_sum(s, kind, j):
        result = r.part[kind, j, mine].astype(F32)
        for slot in (NEAR, ACROSS, OVER):
            scatter(s, kind, j, t, slot).wait_recv()
            result = result + r.arrived[s, kind, j, slot].astype(F32)
        return result

    def scatter_sent(s, kind, j):
        @pl.when(end_chip)
        def _():
            scatter(s, kind, j, over_chip, OVER).wait_send()
            scatter(s, kind, j, near_chip, NEAR).wait_send()

        @pl.when(middle_chip)
        def _():
            scatter(s, kind, j, across_chip, ACROSS).wait_send()

    own_rows = (r.nrm, r.nmlp, r.ups, r.brn, r.act, r.gpre, r.mix, r.dqkv)
    all_rows = (
        r.all_nrm,
        r.all_nmlp,
        r.all_ups,
        r.all_brn,
        r.all_act,
        r.all_gpre,
        r.all_mix,
        r.all_dqkv,
    )

    def rows_copy(index, s, same, stays=False):
        core = c if same else 1 - c
        src = own_rows[index].at[s]
        dst = all_rows[index].at[a, c]
        if index <= BRN:
            src = src.at[:, :, row_block(core, half_width)]
        recv = r.rows_r.at[index]
        if stays:
            return pltpu.make_async_copy(src, dst, recv)
        if same:
            return remote(src, dst, r.rows_s.at[index, s, 0], recv, section=s)
        return remote(src, dst, r.rows_s.at[index, s, 1], recv, section=s, seq=1 - c)

    def rows_start(index, s):
        @pl.when(a == s)
        def _():
            rows_copy(index, s, True, True).start()

        @pl.when(a != s)
        def _():
            rows_copy(index, s, True).start()

        if index <= BRN:
            rows_copy(index, s, False).start()

    def rows_sent(index, s):
        @pl.when(a != s)
        def _():
            rows_copy(index, s, True).wait_send()

        if index <= BRN:
            rows_copy(index, s, False).wait_send()

    def share_copy(index, core):
        view = all_rows[index].at[:, core]
        return remote(view, view, r.share_s.at[index - ACT], r.share_r.at[index - ACT], seq=1 - c)

    def share(index):
        drain(all_rows[index].at[:, c], r.rows_r.at[index])
        share_copy(index, c).start()

    def norm_copy(s):
        return remote(
            r.norm_part.at[s], r.norm_all.at[a], r.norm_s.at[s], r.norm_r, section=s
        )

    def norm_start(s):
        @pl.when(a == s)
        def _():
            pltpu.make_async_copy(r.norm_part.at[s], r.norm_all.at[a], r.norm_r).start()

        @pl.when(a != s)
        def _():
            norm_copy(s).start()

    def home_copy(what, s, chip):
        src, dst, send, recv = what
        return remote(
            src.at[s, chip % 2],
            dst.at[a],
            send.at[s, chip % 2],
            recv,
            section=s,
            tensor=chip,
        )

    def home_start(what, s):
        src, dst, send, recv = what

        @pl.when(middle_chip & (a == s))
        def _():
            pltpu.make_async_copy(src.at[s, t % 2], dst.at[a], recv).start()

        @pl.when(middle_chip & (a != s))
        def _():
            home_copy(what, s, t).start()

        @pl.when(middle_chip)
        def _():
            home_copy(what, s, near_chip).start()

    def home_sent(what, s):
        @pl.when(middle_chip & (a != s))
        def _():
            home_copy(what, s, t).wait_send()

        @pl.when(middle_chip)
        def _():
            home_copy(what, s, near_chip).wait_send()

    out_home = (r.out_low, r.acts, r.out_s, r.out_r)
    grad_home = (r.grad_low, r.grads, r.grad_s, r.grad_r)

    length = r.lengths[a // buckets, a % buckets]
    key = place_of(iota((stream_rows, total), 1))
    for j in streams:
        query = place_of(c * local + j * stream_rows + iota((stream_rows, total), 0))
        r.near[j] = jnp.where((query >= key) & (query - key < WIN), 1.0, 0.0)
    key_row = place_of(iota((1, total), 1))

    def row_mask(place):
        return jnp.where(place < length, 1.0, 0.0)

    def multiplicity(s, j, head):
        far = []
        for block in range(blocks):
            pick = head * blocks + block
            limit = (c * blocks + block) * QB - WIN
            counted = jnp.where(key_row <= limit, r.count[s, pick : pick + 1, :], 0.0)
            far.append(jnp.broadcast_to(counted, (stream_rows // blocks, total)))
        return r.near[j] + jnp.concatenate(far, axis=0)

    def head_cols(head):
        return slice(head * HDIM, (head + 1) * HDIM)

    def kv_copy(s):
        view = r.kv.at[s, :, 0:local]
        return remote(view, view, r.kv_s.at[s], r.kv_r.at[s], seq=1 - c)

    def dkv_copy(s):
        return remote(r.dkv_out.at[s], r.dkv_in.at[s], r.dkv_s.at[s], r.dkv_r.at[s], seq=1 - c)

    def own_sequence(ref):
        both = ref[a // buckets].astype(F32)
        picked = both[:, 0, :]
        for bucket in range(1, buckets):
            picked = jnp.where(a % buckets == bucket, both[:, bucket, :], picked)
        return picked

    def own_part(j):
        chip, first = (j * owned) // rows, (j * owned) % rows
        return chip, slice(first, first + owned)

    def first_copy():
        return remote(r.first_out, r.first_in, r.first_s, r.first_r, tensor=near_chip)

    own_place = c * local + t * rows + iota((rows, 1), 0)
    r.first_out[0] = own_sequence(r.inputs).astype(LOW)
    r.first_out[1] = (own_sequence(r.cotangent) * row_mask(own_place)).astype(LOW)
    r.norm_part[...] = jnp.zeros_like(r.norm_part)

    @pl.when(c == 0)
    def _():
        r.kv[:, :, local:total] = jnp.zeros((lines, 2, local, head_width), LOW)


    @pl.when(end_chip)
    def _():
        first_copy().start()

    @pl.when(middle_chip)
    def _():
        first_copy().wait_recv()
        for which in range(2):
            here, beside_it = r.first_out[which].astype(F32), r.first_in[which].astype(F32)
            lower = jnp.where(t % 2 == 0, here, beside_it)
            upper = jnp.where(t % 2 == 0, beside_it, here)
            for j in streams:
                chip, part = own_part(j)
                own_block = (lower, upper)[chip][part]
                if which == 0:
                    r.hidden[j] = own_block
                else:
                    r.upstream[j] = own_block.astype(LOW)

    def on_owner(stage):
        def run(s, j):
            @pl.when(middle_chip)
            def _():
                stage(s, j)

        return run

    def keep_rows(target, s, j, result):
        chip, part = own_part(j)
        target[s, chip, part] = result

    @on_owner
    def enter(s, j):
        xhat, inverse = standard(r.hidden[j])
        r.xhat1[s, j] = xhat
        r.inv1[s, j] = jnp.broadcast_to(inverse, (owned, 128))
        r.nrm[s, j, mine] = (xhat * r.small[s, 0:1] + r.small[s, 1:2]).astype(LOW)
        gather_start(r.nrm, s, 0, j)

    def project(s, j):
        gather_wait(r.nrm, s, 0, j)
        normed = r.nrm[s, j]
        place = row_block(c * STREAMS + j, stream_rows)
        bias_v = r.small[s, 7:8, half_width : half_width + head_width]
        key_rows = dot_nt(normed, r.wq[s, head_width : 2 * head_width])
        value_rows = dot_nt(normed, r.wq[s, 2 * head_width : 3 * head_width]) + bias_v
        r.kv[s, 0, place] = key_rows.astype(LOW)
        r.kv[s, 1, place] = value_rows.astype(LOW)
        gather_sent(r.nrm, s, 0, j)

    def ask(s, j):
        queries = dot_nt(r.nrm[s, j], r.wq[s, 0:head_width]) + r.small[s, 7:8, :head_width]
        r.qry[s, j] = queries.astype(LOW)

    def attend_line(s, j):
        mixed = []
        for head in range(heads):
            cols = head_cols(head)
            times = multiplicity(s, j, head)
            scores = scale * dot_nt(r.qry[s, j, :, cols], r.kv[s, 0, :, cols])
            scores = jnp.where(times > 0.0, scores, MASKED)
            top = jnp.max(scores, axis=-1, keepdims=True)
            terms = times * jnp.exp(scores - top)
            weights = terms / jnp.sum(terms, axis=-1, keepdims=True)
            r.soft[s, j, head] = weights
            mixed.append(dot_nn(weights.astype(LOW), r.kv[s, 1, :, cols]))
        mask = row_mask(place_of(c * local + j * stream_rows + iota((stream_rows, 1), 0)))
        r.mix[s, j] = (jnp.concatenate(mixed, axis=-1) * mask).astype(LOW)

    def leave_attention(s, j):
        scatter_start(s, 0, j, dot_nn(r.mix[s, j], r.wo[s]))

    @on_owner
    def between(s, j):
        middle = r.hidden[j] + scatter_sum(s, 0, j) + r.small[s, 4:5]
        r.middle[j] = middle
        xhat, inverse = standard(middle)
        r.xhat2[s, j] = xhat
        r.inv2[s, j] = jnp.broadcast_to(inverse, (owned, 128))
        r.nmlp[s, j, mine] = (xhat * r.small[s, 2:3] + r.small[s, 3:4]).astype(LOW)
        gather_start(r.nmlp, s, 1, j)

    def feed(s, j):
        gather_wait(r.nmlp, s, 1, j)
        before = dot_nn(r.nmlp[s, j], r.wf[s]) + r.small[s, 6:7, :units]
        bend = jnp.tanh(0.7978845608028654 * (before + 0.044715 * before * before * before))
        r.act[s, j] = (0.5 * before * (1.0 + bend)).astype(LOW)
        r.slope[s, j] = 0.5 * (1.0 + bend) + 0.5 * before * (1.0 - bend * bend) * (
            0.7978845608028654 * (1.0 + 3 * 0.044715 * before * before)
        )

        gather_sent(r.nmlp, s, 1, j)

    def leave_feed(s, j):
        scatter_start(s, 1, j, dot_nn(r.act[s, j], r.wp[s]))

    @on_owner
    def finish(s, j):
        result = r.middle[j] + scatter_sum(s, 1, j) + r.small[s, 5:6]
        keep_rows(r.out_low, s, j, result.astype(LOW))
        r.hidden[j] = result.astype(LOW).astype(F32)

    def small_ready(s):
        @pl.when(a != s)
        def _():
            small_copy(0, a, s).wait_recv()

    small_ready(0)
    for j in streams:
        enter(0, j)

    def forward(s, _):
        need(s, 0)
        for j in streams:
            project(s, j)

        @pl.when(c == 0)
        def _():
            kv_copy(s).start()

        for j in streams:
            ask(s, j)
        rows_start(NRM, s)

        @pl.when(a != s)
        def _():
            count_copy(0, a, s).wait_recv()

        @pl.when(c == 1)
        def _():
            kv_copy(s).wait_recv()

        for j in streams:
            attend_line(s, j)
            if j == 0:
                need(s, 1)
            leave_attention(s, j)
        rows_start(MIX, s)

        @pl.when(s == 0)
        def _():
            pass_later((0, 1), False)

        @pl.when(s > 0)
        def _():
            pass_far(s, 2)
            pass_far(s, 3)

        for j in streams:
            between(s, j)
            scatter_sent(s, 0, j)
        need(s, 2)

        @pl.when(s == 0)
        def _():
            pass_later((2,), False)

        for j in streams:
            feed(s, j)
            if j == 0:
                need(s, 3)
            leave_feed(s, j)

        @pl.when(s == 0)
        def _():
            pass_later((3,), False)

        rows_start(NMLP, s)
        rows_start(ACT, s)

        @pl.when(s + 1 < lines)
        def _():
            small_ready(s + 1)

        for j in streams:
            finish(s, j)
            scatter_sent(s, 1, j)

            @pl.when(s + 1 < lines)
            def _():
                enter(s + 1, j)

        home_start(out_home, s)

        @pl.when(s == 0)
        def _():
            pass_later(range(4), True)

        @pl.when(s + 1 < lines)
        def _():
            pass_far(s + 1, 0)
            pass_far(s + 1, 1)

        return 0

    lax.fori_loop(0, lines, forward, 0)

    @on_owner
    def turn(s, j):
        upstream = r.upstream[j]
        r.ups[s, j, mine] = upstream
        gather_start(r.ups, s, 2, j)
        r.norm_part[s, 5:6] += column_sum(upstream)

    def feed_back(s, j):
        gather_wait(r.ups, s, 2, j)
        grad_pre = (dot_nt(r.ups[s, j], r.wp[s]) * r.slope[s, j]).astype(LOW)
        r.gpre[s, j] = grad_pre
        scatter_start(s, 2, j, dot_nt(grad_pre, r.wf[s]))
        r.norm_part[s, 6:7, :units] += column_sum(grad_pre)
        gather_sent(r.ups, s, 2, j)

    @on_owner
    def between_back(s, j):
        grad = scatter_sum(s, 2, j)
        xhat = r.xhat2[s, j]
        upstream = r.upstream[j].astype(F32)
        grad_middle = upstream + standard_back(
            grad * r.small[s, 2:3], xhat, r.inv2[s, j, :, 0:1]
        )
        r.middle[j] = grad_middle
        branch = grad_middle.astype(LOW)
        r.brn[s, j, mine] = branch
        gather_start(r.brn, s, 3, j)
        r.norm_part[s, 2:3] += column_sum(grad * xhat)
        r.norm_part[s, 3:4] += column_sum(grad)
        r.norm_part[s, 4:5] += column_sum(branch)

    def mixed_back(s, j):
        gather_wait(r.brn, s, 3, j)
        place = place_of(c * local + j * stream_rows + iota((stream_rows, 1), 0))
        r.gmix[j] = (dot_nt(r.brn[s, j], r.wo[s]) * row_mask(place)).astype(LOW)
        gather_sent(r.brn, s, 3, j)

    def attend_line_back(s, j):
        grad_q, grad_k, grad_v = [], [], []
        for head in range(heads):
            cols = head_cols(head)
            weights = r.soft[s, j, head]
            grad_head = r.gmix[j, :, cols]
            grad_weights = dot_nt(grad_head, r.kv[s, 1, :, cols])
            inner = jnp.sum(weights * grad_weights, axis=-1, keepdims=True)
            grad_scores = (weights * (grad_weights - inner)).astype(LOW)
            grad_k.append(scale * dot_tn(grad_scores, r.qry[s, j, :, cols]))
            grad_v.append(dot_tn(weights.astype(LOW), grad_head))
            grad_q.append(scale * dot_nn(grad_scores, r.kv[s, 0, :, cols]))
        for which, grad in enumerate((grad_k, grad_v)):
            grad = jnp.concatenate(grad, axis=-1)
            r.dkv_all[which] = grad if j == 0 else r.dkv_all[which] + grad
        grad_q = jnp.concatenate(grad_q, axis=-1).astype(LOW)
        r.dqkv[s, 0, j] = grad_q
        r.norm_part[s, 7:8, :head_width] += column_sum(grad_q)

    def join_keys(s):
        @pl.when(c == 1)
        def _():
            r.dkv_out[s] = r.dkv_all[:, 0:local].astype(LOW)
            dkv_copy(s).start()

        @pl.when(c == 0)
        def _():
            dkv_copy(s).wait_recv()
            r.dkv_all[:, 0:local] += r.dkv_in[s].astype(F32)

        for which in range(2):
            joined = r.dkv_all[which, my_half].astype(LOW)
            r.dqkv[s, 1 + which] = joined.reshape(r.dqkv.shape[2:])
            if which == 1:
                r.norm_part[s, 7:8, half_width : half_width + head_width] = column_sum(joined)

    def leave_back(s, j):
        product = dot_nn(r.dqkv[s, 0, j], r.wq[s, 0:head_width])
        for which in range(1, 3):
            weight = r.wq[s, which * head_width : (which + 1) * head_width]
            product = product + dot_nn(r.dqkv[s, which, j], weight)
        scatter_start(s, 3, j, product)

    @on_owner
    def finish_back(s, j):
        grad = scatter_sum(s, 3, j)
        xhat = r.xhat1[s, j]
        result = r.middle[j] + standard_back(
            grad * r.small[s, 0:1], xhat, r.inv1[s, j, :, 0:1]
        )
        r.upstream[j] = result.astype(LOW)
        keep_rows(r.grad_low, s, j, result.astype(LOW))
        r.norm_part[s, 0:1] += column_sum(grad * xhat)
        r.norm_part[s, 1:2] += column_sum(grad)

    for j in streams:
        turn(lines - 1, j)

    def backward(index, _):
        s = lines - 1 - index
        for j in streams:
            feed_back(s, j)
        rows_start(UPS, s)
        rows_start(GPRE, s)

        @pl.when(index == 1)
        def _():
            share(ACT)
            share(MIX)

        for j in streams:
            between_back(s, j)
            scatter_sent(s, 2, j)
        for j in streams:
            mixed_back(s, j)
            attend_line_back(s, j)
        join_keys(s)
        rows_start(BRN, s)
        for j in streams:
            leave_back(s, j)
        rows_start(DQKV, s)
        for j in streams:
            finish_back(s, j)
            scatter_sent(s, 3, j)

            @pl.when(s > 0)
            def _():
                turn(s - 1, j)

        norm_start(s)
        home_start(grad_home, s)
        return 0

    lax.fori_loop(0, lines, backward, 0)

    share(GPRE)
    share(DQKV)

    drain(r.norm_all, r.norm_r)
    slot = c * chips + t
    norm_sum = r.norm_all[0]
    for line in range(1, lines):
        norm_sum = norm_sum + r.norm_all[line]
    r.ends[slot] = norm_sum

    def ends_copy(step):
        core, chip = step // chips, step % chips
        view = r.ends.at[slot]
        return remote(
            view,
            view,
            r.ends_s.at[step - 1],
            r.ends_r,
            seq=(c + core) % 2,
            tensor=(t + chip) % chips,
        )

    for step in range(1, 2 * chips):
        ends_copy(step).start()

    for index in range(ACT):
        drain(all_rows[index], r.rows_r.at[index])
    for index in range(ACT, 8):
        share_copy(index, 1 - c).wait_recv()
        share_copy(index, c).wait_send()
    drain(r.acts, r.out_r)
    drain(r.grads, r.grad_r)
    drain(r.ends.at[0 : 2 * chips - 1], r.ends_r)
    for step in range(1, 2 * chips):
        ends_copy(step).wait_send()
    for step in range(1, lines):
        small_copy(step - 1, (a + step) % lines, a).wait_send()
        count_copy(step - 1, (a + step) % lines, a).wait_send()
    for p in range(4):
        for which, line in enumerate((beside(a), above(a))):
            first_hop(p, a, line, which).wait_send()

    @pl.when(end_chip)
    def _():
        first_copy().wait_send()

    def sent(s, _):
        home_sent(out_home, s)
        home_sent(grad_home, s)

        @pl.when(a != s)
        def _():
            norm_copy(s).wait_send()

        @pl.when(c == 0)
        def _():
            kv_copy(s).wait_send()

        @pl.when(c == 1)
        def _():
            dkv_copy(s).wait_send()

        for index in range(8):
            rows_sent(index, s)
        for p in range(4):

            @pl.when((a == beside(s)) | (a == above(s)))
            def _():
                second_hop(p, s, 0).wait_send()

            @pl.when(a != s)
            def _():
                core_hop(p, s, c).wait_send()

        return 0

    lax.fori_loop(0, lines, sent, 0)


def relay_call(inputs, cotangent, lengths, chosen, singles, weights):
    lines = lax.axis_size("section")
    chips = lax.axis_size("tensor")
    rows, buckets, width = inputs.shape[1:]
    local, total, half = rows * chips, 2 * rows * chips, width // 2
    head_width, units = weights["wo_in"].shape[0], weights["wp_in"].shape[0]
    heads = head_width // HDIM
    stream = local // STREAMS
    peers, owned = chips - 1, stream // 2
    vmem, dma = pltpu.VMEM, pltpu.SemaphoreType.DMA
    operands = dict(
        inputs=inputs,
        cotangent=cotangent,
        lengths=lengths,
        chosen=chosen,
        **singles,
        **weights,
    )

    def space(name):
        if name in weights:
            return pl.ANY
        return pltpu.SMEM if operands[name] is lengths else pltpu.VMEM

    sums = dict(
        acts=((lines, rows, width), LOW),
        grads=((lines, rows, width), LOW),
        ends=((2 * chips, 8, width), F32),
    )
    gathered = dict(
        all_nrm=((lines, 2, STREAMS, stream, half), LOW),
        all_nmlp=((lines, 2, STREAMS, stream, half), LOW),
        all_ups=((lines, 2, STREAMS, stream, half), LOW),
        all_brn=((lines, 2, STREAMS, stream, half), LOW),
        all_act=((lines, 2, STREAMS, stream, units), LOW),
        all_gpre=((lines, 2, STREAMS, stream, units), LOW),
        all_mix=((lines, 2, STREAMS, stream, head_width), LOW),
        all_dqkv=((lines, 2, 3, STREAMS, stream, head_width), LOW),
    )
    outputs = dict(**sums, **gathered)
    scratch = dict(
        wq=vmem((lines,) + weights["wq_in"].shape, LOW),
        wo=vmem((lines,) + weights["wo_in"].shape, LOW),
        wf=vmem((lines,) + weights["wf_in"].shape, LOW),
        wp=vmem((lines,) + weights["wp_in"].shape, LOW),
        small_own=vmem((8, width), F32),
        small=vmem((lines, 8, width), F32),
        count_own=vmem((lines, 8, total), F32),
        count=vmem((lines, 8, total), F32),
        hidden=vmem((STREAMS, owned, width), F32),
        middle=vmem((STREAMS, owned, width), F32),
        upstream=vmem((STREAMS, owned, width), LOW),
        first_out=vmem((2, rows, width), LOW),
        first_in=vmem((2, rows, width), LOW),
        xhat1=vmem((lines, STREAMS, owned, width), F32),
        inv1=vmem((lines, STREAMS, owned, 128), F32),
        xhat2=vmem((lines, STREAMS, owned, width), F32),
        inv2=vmem((lines, STREAMS, owned, 128), F32),
        nrm=vmem((lines, STREAMS, stream, width), LOW),
        nmlp=vmem((lines, STREAMS, stream, width), LOW),
        ups=vmem((lines, STREAMS, stream, width), LOW),
        brn=vmem((lines, STREAMS, stream, width), LOW),
        act=vmem((lines, STREAMS, stream, units), LOW),
        gpre=vmem((lines, STREAMS, stream, units), LOW),
        slope=vmem((lines, STREAMS, stream, units), F32),
        mix=vmem((lines, STREAMS, stream, head_width), LOW),
        qry=vmem((lines, STREAMS, stream, head_width), LOW),
        gmix=vmem((STREAMS, stream, head_width), LOW),
        dqkv=vmem((lines, 3, STREAMS, stream, head_width), LOW),
        kv=vmem((lines, 2, total, head_width), LOW),
        soft=vmem((lines, STREAMS, heads, stream, total), F32),
        near=vmem((STREAMS, stream, total), F32),
        dkv_all=vmem((2, total, head_width), F32),
        dkv_out=vmem((lines, 2, local, head_width), LOW),
        dkv_in=vmem((lines, 2, local, head_width), LOW),
        part=vmem((4, STREAMS, stream, width), LOW),
        arrived=vmem((lines, 4, STREAMS, peers, owned, width), LOW),
        out_low=vmem((lines, 2, rows, width), LOW),
        grad_low=vmem((lines, 2, rows, width), LOW),
        norm_part=vmem((lines, 8, width), F32),
        norm_all=vmem((lines, 8, width), F32),
        w_first_s=dma((4, 2)),
        w_first_r=dma((lines, 4)),
        w_second_s=dma((lines, 4)),
        w_second_r=dma((lines, 4, 2)),
        w_core_s=dma((lines, 4)),
        w_core_r=dma((lines, 4)),
        w_own=dma((4,)),
        small_s=dma((lines - 1,)),
        small_r=dma((lines,)),
        count_s=dma((lines - 1,)),
        count_r=dma((lines,)),
        ag_s=dma((4, STREAMS, peers)),
        ag_r=dma((4, STREAMS, peers)),
        rs_s=dma((4, STREAMS, peers)),
        rs_r=dma((4, STREAMS, peers)),
        kv_s=dma((lines,)),
        kv_r=dma((lines,)),
        dkv_s=dma((lines,)),
        dkv_r=dma((lines,)),
        rows_s=dma((8, lines, 2)),
        rows_r=dma((8,)),
        share_s=dma((4,)),
        share_r=dma((4,)),
        first_s=dma,
        first_r=dma,
        out_s=dma((lines, 2)),
        out_r=dma,
        grad_s=dma((lines, 2)),
        grad_r=dma,
        norm_s=dma((lines,)),
        norm_r=dma,
        ends_s=dma((2 * chips - 1,)),
        ends_r=dma,
    )
    names = tuple(operands) + tuple(outputs) + tuple(scratch)
    results = pl.pallas_call(
        functools.partial(relay_kernel, names),
        out_shape=[jax.ShapeDtypeStruct(shape, kind) for shape, kind in outputs.values()],
        in_specs=[pl.BlockSpec(memory_space=space(name)) for name in operands],
        out_specs=[
            pl.BlockSpec(memory_space=pl.ANY if name in gathered else pltpu.VMEM)
            for name in outputs
        ],
        scratch_shapes=list(scratch.values()),
        compiler_params=pltpu.CompilerParams(
            collective_id=0, has_side_effects=True, vmem_limit_bytes=60 * 2**20
        ),
        name="relay",
    )(*operands.values())
    return dict(zip(outputs, results))


def weights_kernel(names, *refs):
    r = types.SimpleNamespace(**dict(zip(names, refs)))
    step = pl.program_id(0)
    micro_count, rows, buckets, width = r.activations.shape
    chips, units, head_width = r.ends.shape[0] // 2, r.all_act.shape[-1], r.all_mix.shape[-1]

    @pl.when(step == 0)
    def _():
        sums = r.ends[0]
        for other in range(1, 2 * chips):
            sums = sums + r.ends[other]
        singles = (r.ln1_gain, r.ln1_shift, r.ln2_gain, r.ln2_shift, r.b_out, r.b_proj)
        for place, single in enumerate(singles):
            single[...] = sums[place : place + 1]
        for chip in range(chips):
            both = r.ends[chip] + r.ends[chips + chip]
            r.b_fc[:, chip * units : (chip + 1) * units] = both[6:7, :units]
            here = slice(chip * head_width, (chip + 1) * head_width)
            r.b_qv[0:1, here] = both[7:8, :head_width]
            r.b_qv[1:2, here] = both[7:8, width // 2 : width // 2 + head_width]
        for target, source in ((r.activations, r.acts), (r.in_grads, r.grads)):
            for micro in range(micro_count):
                rows_of = [
                    source[micro * buckets + bucket].astype(F32)[:, None, :]
                    for bucket in range(buckets)
                ]
                target[micro] = jnp.concatenate(rows_of, axis=1).astype(LOW)
        for target in (r.w_qkv, r.w_out, r.w_fc, r.w_proj):
            target[...] = jnp.zeros_like(target)

    def rows_of_sequence(ref):
        return ref[0].reshape(2 * chips * rows, ref.shape[-1])

    nrm, nmlp, ups, brn, act, gpre, mix = (
        rows_of_sequence(ref)
        for ref in (r.all_nrm, r.all_nmlp, r.all_ups, r.all_brn, r.all_act, r.all_gpre, r.all_mix)
    )
    r.w_proj[...] += dot_tn(act, ups)
    r.w_fc[...] += dot_tn(nmlp, gpre)
    r.w_out[...] += dot_tn(mix, brn)
    for which in range(3):
        grad = r.all_dqkv[0, :, which].reshape(2 * chips * rows, head_width)
        r.w_qkv[which] += dot_tn(grad, nrm)


def weights_call(relayed, inputs_shape, head_width, units):
    lines = lax.axis_size("section")
    chips = lax.axis_size("tensor")
    width = inputs_shape[-1]
    half = width // 2
    outputs = dict(
        activations=(inputs_shape, LOW),
        in_grads=(inputs_shape, LOW),
        ln1_gain=((1, width), F32),
        ln1_shift=((1, width), F32),
        w_qkv=((3, head_width, half), F32),
        b_qv=((2, width), F32),
        w_out=((head_width, half), F32),
        b_out=((1, width), F32),
        ln2_gain=((1, width), F32),
        ln2_shift=((1, width), F32),
        w_fc=((half, units), F32),
        b_fc=((1, chips * units), F32),
        w_proj=((units, half), F32),
        b_proj=((1, width), F32),
    )

    def spec(array):
        if len(array.shape) < 5:
            return pl.BlockSpec(array.shape, lambda step: (0,) * len(array.shape))
        return pl.BlockSpec(
            (1,) + array.shape[1:], lambda step: (step,) + (0,) * (len(array.shape) - 1)
        )

    def whole(shape):
        return pl.BlockSpec(shape, lambda step: (0,) * len(shape))

    return pl.pallas_call(
        functools.partial(weights_kernel, tuple(relayed) + tuple(outputs)),
        out_shape=[jax.ShapeDtypeStruct(shape, kind) for shape, kind in outputs.values()],
        grid=(lines,),
        in_specs=[spec(array) for array in relayed.values()],
        out_specs=[whole(shape) for shape, _ in outputs.values()],
        compiler_params=pltpu.CompilerParams(vmem_limit_bytes=60 * 2**20),
        name="weight_gradients",
    )(*relayed.values())


def on_line(
    inputs,
    cotangent,
    lengths,
    chosen,
    ln1_gain,
    ln1_shift,
    w_qkv,
    b_qv,
    w_out,
    b_out,
    ln2_gain,
    ln2_shift,
    w_fc,
    b_fc,
    w_proj,
    b_proj,
):
    head_width, units = w_out.shape[1], w_fc.shape[2]
    singles = dict(
        ln1_gain=ln1_gain,
        ln1_shift=ln1_shift,
        ln2_gain=ln2_gain,
        ln2_shift=ln2_shift,
        b_out=b_out,
        b_proj=b_proj,
        b_fc=b_fc,
        b_qv=b_qv[0],
    )
    weights = dict(
        wq_in=jnp.swapaxes(w_qkv[0], 1, 2).reshape(-1, inputs.shape[-1]),
        wo_in=w_out[0],
        wf_in=w_fc[0],
        wp_in=w_proj[0],
    )
    picks = chosen.reshape((-1,) + chosen.shape[-2:])
    relayed = relay_call(inputs, cotangent, lengths, picks, singles, weights)
    results = list(weights_call(relayed, inputs.shape, head_width, units))
    results[4] = jnp.swapaxes(results[4], 1, 2)
    vectors = (2, 3, 7, 8, 9, 11, 13)
    return tuple(
        result if place in vectors else result[None] for place, result in enumerate(results)
    )


def fits_lines(mesh):
    return mesh.shape["section"] == 4 and mesh.shape["seq"] == 2 and mesh.shape["tensor"] == 4


def solution(mesh):
    placed = (
        P(None, ("seq", "tensor"), None, None),
        P(None, ("seq", "tensor"), None, None),
        P(),
        P("section", None, None, "tensor", "seq", None),
        P("section", None),
        P("section", None),
        P("section", None, None, "tensor"),
        P("section", None, "tensor"),
        P("section", "tensor", None),
        P("section", None),
        P("section", None),
        P("section", None),
        P("section", None, "tensor"),
        P("section", "tensor"),
        P("section", "tensor", None),
        P("section", None),
    )
    return jax.shard_map(
        on_line if fits_lines(mesh) else on_device,
        mesh=mesh,
        in_specs=placed,
        out_specs=(
            P("section", None, ("seq", "tensor"), None, None),
            P("section", None, ("seq", "tensor"), None, None),
            P("section", None),
            P("section", None),
            P("section", None, "seq", "tensor"),
            P("section", None, None),
            P("section", "tensor", "seq"),
            P("section", None),
            P("section", None),
            P("section", None),
            P("section", "seq", "tensor"),
            P("section", None),
            P("section", "tensor", "seq"),
            P("section", None),
        ),
        check_vma=False,
    )
```

```python
import functools
import types

import jax
import jax.numpy as jnp
from jax import lax
from jax.experimental import pallas as pl
from jax.experimental.pallas import tpu as pltpu
from jax.sharding import PartitionSpec as P

HDIM = 64
WIN = 64
QB = 64
KSEL = 64


NORM_EPS = 1e-05
MASKED = -1000000000.0


def from_behind(value, axis, steps):
    count = lax.axis_size(axis)
    first, last = (max(0, -steps), min(count, count - steps))
    return lax.ppermute(value, axis, [(source, source + steps) for source in range(first, last)])


def layer_norm(values, gain, shift):
    average = jnp.mean(values, axis=-1, keepdims=True)
    centred = values - average
    variance = jnp.mean(centred * centred, axis=-1, keepdims=True)
    return centred * lax.rsqrt(variance + NORM_EPS) * gain + shift


def gelu_tanh(values):
    return (
        0.5
        * values
        * (1.0 + jnp.tanh(0.7978845608028654 * (values + 0.044715 * values * values * values)))
    )


def gather_rows(row_block):
    return lax.all_gather(row_block, "tensor", axis=0, tiled=True)


def scatter_product(left_rows, weight, formula):
    return lax.psum_scatter(
        jnp.einsum(formula, left_rows, weight, preferred_element_type=jnp.float32).astype(
            jnp.bfloat16
        ),
        "tensor",
        scatter_dimension=0,
        tiled=True,
    ).astype(jnp.float32)


def near_slabs(full_rows, seq_start, seq_first, length_local):
    buckets = full_rows.shape[1]
    heads_local = full_rows.shape[2] // HDIM
    blocks = length_local // QB
    earlier = lax.dynamic_slice_in_dim(full_rows, jnp.maximum(seq_start - WIN, 0), WIN, 0)
    earlier = jnp.where(seq_first, jnp.zeros_like(earlier), earlier)
    local_part = lax.dynamic_slice_in_dim(full_rows, seq_start, length_local, 0)
    segment = jnp.concatenate([earlier, local_part], 0).reshape(
        length_local + WIN, buckets, heads_local, HDIM
    )
    return jnp.concatenate(
        [
            segment[offset_index * QB : offset_index * QB + length_local].reshape(
                blocks, QB, buckets, heads_local, HDIM
            )
            for offset_index in range(WIN // QB + 1)
        ],
        1,
    )


def far_rows(full_rows, flat_index):
    total_rows, buckets, feature_width = full_rows.shape
    heads_local = feature_width // HDIM
    return jnp.take(full_rows.reshape(total_rows * buckets * heads_local, HDIM), flat_index, axis=0)


def key_geometry(chosen_now, seq_start, blocks):
    buckets, heads_local = (chosen_now.shape[0], chosen_now.shape[1])
    bucket_ids = lax.broadcasted_iota(jnp.int32, chosen_now.shape, 0)
    head_ids = lax.broadcasted_iota(jnp.int32, chosen_now.shape, 1)
    flat_index = (chosen_now * buckets + bucket_ids) * heads_local + head_ids
    block_start = seq_start + QB * lax.broadcasted_iota(jnp.int32, (blocks, 1, 1), 0)
    query_ids = lax.broadcasted_iota(jnp.int32, (1, QB, 1), 1)
    key_ids = lax.broadcasted_iota(jnp.int32, (1, 1, WIN + QB), 2)
    distance = query_ids + WIN - key_ids
    near_ok = (distance >= 0) & (distance < WIN) & (block_start + key_ids - WIN >= 0)
    far_ok = chosen_now + WIN <= block_start.reshape(1, 1, blocks, 1)
    near_mask = jnp.broadcast_to(
        near_ok[:, None, None], (blocks, buckets, heads_local, QB, WIN + QB)
    )
    far_mask = jnp.broadcast_to(
        jnp.transpose(far_ok, (2, 0, 1, 3))[:, :, :, None, :],
        (blocks, buckets, heads_local, QB, KSEL),
    )
    return (flat_index, jnp.concatenate([near_mask, far_mask], -1))


def attention_setup(queries, key_rows, value_rows, chosen_now, seq_start, seq_first):
    length_local, buckets, feature_width = queries.shape
    heads_local = feature_width // HDIM
    blocks = length_local // QB
    query_blocks = queries.reshape(blocks, QB, buckets, heads_local, HDIM)
    flat_index, key_mask = key_geometry(chosen_now, seq_start, blocks)
    near_keys = near_slabs(key_rows, seq_start, seq_first, length_local)
    near_values = near_slabs(value_rows, seq_start, seq_first, length_local)
    far_keys = far_rows(key_rows, flat_index)
    far_values = far_rows(value_rows, flat_index)
    near_scores = jnp.einsum(
        "bqnhe,btnhe->bnhqt", query_blocks, near_keys, preferred_element_type=jnp.float32
    )
    far_scores = jnp.einsum(
        "bqnhe,nhbke->bnhqk", query_blocks, far_keys, preferred_element_type=jnp.float32
    )
    scores = jnp.where(
        key_mask, HDIM ** (-0.5) * jnp.concatenate([near_scores, far_scores], -1), MASKED
    )
    return (query_blocks, near_keys, near_values, far_keys, far_values, flat_index, scores)


def attend(queries, key_rows, value_rows, chosen_now, seq_start, seq_first):
    query_blocks, near_keys, near_values, far_keys, far_values, flat_index, scores = (
        attention_setup(queries, key_rows, value_rows, chosen_now, seq_start, seq_first)
    )
    span = WIN + QB
    row_top = jnp.max(scores, -1, keepdims=True)
    exp_terms = jnp.exp(scores - row_top)
    row_total = jnp.sum(exp_terms, -1, keepdims=True)
    softmax_low = (exp_terms / row_total).astype(jnp.bfloat16)
    near_part = jnp.einsum(
        "bnhqt,btnhe->bqnhe",
        softmax_low[..., :span],
        near_values,
        preferred_element_type=jnp.float32,
    )
    far_part = jnp.einsum(
        "bnhqk,nhbke->bqnhe",
        softmax_low[..., span:],
        far_values,
        preferred_element_type=jnp.float32,
    )
    return ((near_part + far_part).reshape(queries.shape), row_top + jnp.log(row_total))


def spread_back(near_grad, far_grad, flat_index, seq_start, seq_first, total_rows):
    blocks, span, buckets, heads_local, head_size = near_grad.shape
    length_local = blocks * QB
    feature_width = heads_local * head_size
    segment = jnp.zeros((length_local + WIN, buckets, heads_local, head_size), jnp.float32)
    for offset_index in range(WIN // QB + 1):
        piece = near_grad[:, offset_index * QB : (offset_index + 1) * QB].reshape(
            length_local, buckets, heads_local, head_size
        )
        segment = segment.at[offset_index * QB : offset_index * QB + length_local].add(piece)
    full_rows = jnp.zeros((total_rows * buckets * heads_local, head_size), jnp.float32)
    full_rows = full_rows.at[flat_index.reshape(-1)].add(far_grad.reshape(-1, head_size))
    full_rows = full_rows.reshape(total_rows, buckets, feature_width)
    local_part = segment[WIN:].reshape(length_local, buckets, feature_width)
    earlier = jnp.where(seq_first, 0.0, segment[:WIN].reshape(WIN, buckets, feature_width))
    full_rows = lax.dynamic_update_slice_in_dim(
        full_rows,
        lax.dynamic_slice_in_dim(full_rows, seq_start, length_local, 0) + local_part,
        seq_start,
        0,
    )
    earlier_start = jnp.maximum(seq_start - WIN, 0)
    full_rows = lax.dynamic_update_slice_in_dim(
        full_rows,
        lax.dynamic_slice_in_dim(full_rows, earlier_start, WIN, 0) + earlier,
        earlier_start,
        0,
    )
    return full_rows


def attend_back(
    queries, key_rows, value_rows, chosen_now, seq_start, seq_first, log_total, grad_mixed
):
    query_blocks, near_keys, near_values, far_keys, far_values, flat_index, scores = (
        attention_setup(queries, key_rows, value_rows, chosen_now, seq_start, seq_first)
    )
    span = WIN + QB
    score_scale = HDIM ** (-0.5)
    grad_blocks = grad_mixed.reshape(query_blocks.shape)
    weights_full = jnp.exp(scores - log_total)
    softmax_low = weights_full.astype(jnp.bfloat16)
    grad_near_weights = jnp.einsum(
        "bqnhe,btnhe->bnhqt", grad_blocks, near_values, preferred_element_type=jnp.float32
    )
    grad_far_weights = jnp.einsum(
        "bqnhe,nhbke->bnhqk", grad_blocks, far_values, preferred_element_type=jnp.float32
    )
    grad_weights = jnp.concatenate([grad_near_weights, grad_far_weights], -1)
    row_dot = jnp.sum(weights_full * grad_weights, -1, keepdims=True)
    grad_scores = (weights_full * (grad_weights - row_dot)).astype(jnp.bfloat16)
    grad_near, grad_far = (grad_scores[..., :span], grad_scores[..., span:])
    grad_queries = score_scale * (
        jnp.einsum("bnhqt,btnhe->bqnhe", grad_near, near_keys, preferred_element_type=jnp.float32)
        + jnp.einsum("bnhqk,nhbke->bqnhe", grad_far, far_keys, preferred_element_type=jnp.float32)
    )
    near_key_grad = score_scale * jnp.einsum(
        "bnhqt,bqnhe->btnhe", grad_near, query_blocks, preferred_element_type=jnp.float32
    )
    far_key_grad = score_scale * jnp.einsum(
        "bnhqk,bqnhe->nhbke", grad_far, query_blocks, preferred_element_type=jnp.float32
    )
    near_value_grad = jnp.einsum(
        "bnhqt,bqnhe->btnhe",
        softmax_low[..., :span],
        grad_blocks,
        preferred_element_type=jnp.float32,
    )
    far_value_grad = jnp.einsum(
        "bnhqk,bqnhe->nhbke",
        softmax_low[..., span:],
        grad_blocks,
        preferred_element_type=jnp.float32,
    )
    total_rows = key_rows.shape[0]
    key_grad = spread_back(
        near_key_grad, far_key_grad, flat_index, seq_start, seq_first, total_rows
    )
    value_grad = spread_back(
        near_value_grad, far_value_grad, flat_index, seq_start, seq_first, total_rows
    )
    return (grad_queries.reshape(queries.shape), key_grad, value_grad)


def forward_pass(hidden, params, chosen_now, query_mask, seq_start, seq_first, finish):
    (
        ln1_gain,
        ln1_shift,
        w_qkv,
        b_qv,
        w_out,
        b_out,
        ln2_gain,
        ln2_shift,
        w_fc,
        b_fc,
        w_proj,
        b_proj,
    ) = params
    hidden_wide = hidden.astype(jnp.float32)
    normed_all = gather_rows(layer_norm(hidden_wide, ln1_gain, ln1_shift).astype(jnp.bfloat16))
    projected = jnp.einsum("pnd,jdc->jpnc", normed_all, w_qkv, preferred_element_type=jnp.float32)
    queries = (projected[0] + b_qv[0]).astype(jnp.bfloat16)
    key_rows, value_rows = (
        lax.all_gather(projected[1].astype(jnp.bfloat16), "seq", axis=0, tiled=True),
        lax.all_gather((projected[2] + b_qv[1]).astype(jnp.bfloat16), "seq", axis=0, tiled=True),
    )
    attended, log_total = attend(queries, key_rows, value_rows, chosen_now, seq_start, seq_first)
    mixed_rows = (attended * query_mask[:, :, None]).astype(jnp.bfloat16)
    middle = hidden_wide + scatter_product(mixed_rows, w_out, "pnc,cd->pnd") + b_out
    normed_mlp = gather_rows(layer_norm(middle, ln2_gain, ln2_shift).astype(jnp.bfloat16))
    pre_active = (
        jnp.einsum("pnd,df->pnf", normed_mlp, w_fc, preferred_element_type=jnp.float32) + b_fc
    )
    active = gelu_tanh(pre_active).astype(jnp.bfloat16)
    if not finish:
        return (
            normed_all,
            queries,
            key_rows,
            value_rows,
            log_total,
            mixed_rows,
            middle,
            normed_mlp,
            pre_active,
            active,
        )
    output = (middle + scatter_product(active, w_proj, "pnf,fd->pnd") + b_proj).astype(jnp.bfloat16)
    return (output, (key_rows, value_rows))


def backward_pass(hidden, upstream, params, chosen_now, query_mask, seq_start, seq_first):
    (
        ln1_gain,
        ln1_shift,
        w_qkv,
        b_qv,
        w_out,
        b_out,
        ln2_gain,
        ln2_shift,
        w_fc,
        b_fc,
        w_proj,
        b_proj,
    ) = params
    (
        normed_all,
        queries,
        key_rows,
        value_rows,
        log_total,
        mixed_rows,
        middle,
        normed_mlp,
        pre_active,
        active,
    ) = forward_pass(hidden, params, chosen_now, query_mask, seq_start, seq_first, False)
    upstream_all = gather_rows(upstream)
    grad_w_proj = jnp.einsum(
        "pnf,pnd->fd", active, upstream_all, preferred_element_type=jnp.float32
    )
    grad_b_proj = jnp.sum(upstream.astype(jnp.float32), axis=(0, 1))
    grad_active = jnp.einsum(
        "pnd,fd->pnf", upstream_all, w_proj, preferred_element_type=jnp.float32
    )
    unused_value, gelu_pull = jax.vjp(gelu_tanh, pre_active)
    grad_pre = gelu_pull(grad_active)[0].astype(jnp.bfloat16)
    grad_w_fc = jnp.einsum("pnd,pnf->df", normed_mlp, grad_pre, preferred_element_type=jnp.float32)
    grad_b_fc = jnp.sum(grad_pre.astype(jnp.float32), axis=(0, 1))
    grad_normed_mlp = scatter_product(grad_pre, w_fc, "pnf,df->pnd")
    unused_norm, second_pull = jax.vjp(layer_norm, middle, ln2_gain, ln2_shift)
    grad_mid_norm, grad_ln2_gain, grad_ln2_shift = second_pull(grad_normed_mlp)
    grad_middle = upstream.astype(jnp.float32) + grad_mid_norm
    grad_branch = grad_middle.astype(jnp.bfloat16)
    grad_b_out = jnp.sum(grad_branch.astype(jnp.float32), axis=(0, 1))
    branch_all = gather_rows(grad_branch)
    grad_w_out = jnp.einsum(
        "pnc,pnd->cd", mixed_rows, branch_all, preferred_element_type=jnp.float32
    )
    grad_mixed = jnp.einsum(
        "pnd,cd->pnc", branch_all, w_out, preferred_element_type=jnp.float32
    ).astype(jnp.bfloat16) * query_mask[:, :, None].astype(jnp.bfloat16)
    grad_queries, key_grad_all, value_grad_all = attend_back(
        queries, key_rows, value_rows, chosen_now, seq_start, seq_first, log_total, grad_mixed
    )
    key_grad, value_grad = (
        lax.psum_scatter(
            key_grad_all.astype(jnp.bfloat16), "seq", scatter_dimension=0, tiled=True
        ).astype(jnp.float32),
        lax.psum_scatter(
            value_grad_all.astype(jnp.bfloat16), "seq", scatter_dimension=0, tiled=True
        ).astype(jnp.float32),
    )
    grad_project = jnp.stack(
        [
            grad_queries.astype(jnp.bfloat16),
            key_grad.astype(jnp.bfloat16),
            value_grad.astype(jnp.bfloat16),
        ],
        2,
    )
    grad_w_qkv = jnp.einsum(
        "pnd,pnjc->jdc", normed_all, grad_project, preferred_element_type=jnp.float32
    )
    grad_b_qv = jnp.sum(grad_project[:, :, 0::2].astype(jnp.float32), axis=(0, 1))
    grad_normed = scatter_product(grad_project, w_qkv, "pnjc,jdc->pnd")
    unused_first, first_pull = jax.vjp(layer_norm, hidden.astype(jnp.float32), ln1_gain, ln1_shift)
    grad_in_norm, grad_ln1_gain, grad_ln1_shift = first_pull(grad_normed)
    grad_hidden = (grad_middle + grad_in_norm).astype(jnp.bfloat16)
    block_grads = (
        grad_ln1_gain,
        grad_ln1_shift,
        grad_w_qkv,
        grad_b_qv,
        grad_w_out,
        grad_b_out,
        grad_ln2_gain,
        grad_ln2_shift,
        grad_w_fc,
        grad_b_fc,
        grad_w_proj,
        grad_b_proj,
    )
    return (grad_hidden, block_grads)


def on_device(
    inputs,
    cotangent,
    lengths,
    chosen,
    ln1_gain,
    ln1_shift,
    w_qkv,
    b_qv,
    w_out,
    b_out,
    ln2_gain,
    ln2_shift,
    w_fc,
    b_fc,
    w_proj,
    b_proj,
):
    params = tuple(
        (
            weight_array[0]
            for weight_array in (
                ln1_gain,
                ln1_shift,
                w_qkv,
                b_qv,
                w_out,
                b_out,
                ln2_gain,
                ln2_shift,
                w_fc,
                b_fc,
                w_proj,
                b_proj,
            )
        )
    )
    section_index = lax.axis_index("section")
    section_count = lax.axis_size("section")
    seq_index = lax.axis_index("seq")
    tensor_index = lax.axis_index("tensor")
    tensor_count = lax.axis_size("tensor")
    micro_count, rows_local, buckets, feature_width = inputs.shape
    length_local = rows_local * tensor_count
    heads_width = w_qkv.shape[-1]
    seq_start = seq_index * length_local
    seq_first = seq_index == 0
    positions = seq_start + lax.broadcasted_iota(jnp.int32, (micro_count, length_local, buckets), 1)
    mask_all = (positions < lengths[:, None, :]).astype(jnp.float32)
    mask_rows = lax.dynamic_slice_in_dim(mask_all, tensor_index * rows_local, rows_local, 1)
    step_count = micro_count + section_count - 1
    chosen_section = chosen[0]
    received = jnp.zeros((rows_local, buckets, feature_width), jnp.bfloat16)
    stored = jnp.zeros((micro_count, rows_local, buckets, feature_width), jnp.bfloat16)
    outputs = jnp.zeros_like(stored)
    for step_index in range(step_count):
        micro_index = step_index - section_index
        running = (micro_index >= 0) & (micro_index < micro_count)
        slot_index = jnp.clip(micro_index, 0, micro_count - 1)
        block_in = jnp.where(
            section_index == 0, lax.dynamic_index_in_dim(inputs, slot_index, 0, False), received
        )
        chosen_now = lax.dynamic_index_in_dim(chosen_section, slot_index, 0, False)
        query_mask = lax.dynamic_index_in_dim(mask_all, slot_index, 0, False)
        result, key_pair = forward_pass(
            block_in, params, chosen_now, query_mask, seq_start, seq_first, True
        )
        stored = jnp.where(
            running, lax.dynamic_update_index_in_dim(stored, block_in, slot_index, 0), stored
        )
        outputs = jnp.where(
            running, lax.dynamic_update_index_in_dim(outputs, result, slot_index, 0), outputs
        )
        received = from_behind(result, "section", 1)
    back_received = jnp.zeros((rows_local, buckets, feature_width), jnp.bfloat16)
    in_grads = jnp.zeros_like(stored)
    totals = None
    for step_index in range(step_count):
        micro_index = step_index - (section_count - 1 - section_index)
        running = (micro_index >= 0) & (micro_index < micro_count)
        slot_index = jnp.clip(micro_index, 0, micro_count - 1)
        chosen_now = lax.dynamic_index_in_dim(chosen_section, slot_index, 0, False)
        query_mask = lax.dynamic_index_in_dim(mask_all, slot_index, 0, False)
        local_mask = lax.dynamic_index_in_dim(mask_rows, slot_index, 0, False)
        top_grad = (
            lax.dynamic_index_in_dim(cotangent, slot_index, 0, False).astype(jnp.float32)
            * local_mask[:, :, None]
        ).astype(jnp.bfloat16)
        upstream = jnp.where(section_index == section_count - 1, top_grad, back_received)
        hidden = lax.dynamic_index_in_dim(stored, slot_index, 0, False)
        grad_hidden, block_grads = backward_pass(
            hidden, upstream, params, chosen_now, query_mask, seq_start, seq_first
        )
        block_grads = tuple(
            (jnp.where(running, grad_part, jnp.zeros_like(grad_part)) for grad_part in block_grads)
        )
        totals = (
            block_grads
            if step_index == 0
            else tuple(
                (total_part + grad_part for total_part, grad_part in zip(totals, block_grads))
            )
        )
        in_grads = jnp.where(
            running, lax.dynamic_update_index_in_dim(in_grads, grad_hidden, slot_index, 0), in_grads
        )
        back_received = from_behind(grad_hidden, "section", -1)
    (
        sum_ln1_gain,
        sum_ln1_shift,
        sum_w_qkv,
        sum_b_qv,
        sum_w_out,
        sum_b_out,
        sum_ln2_gain,
        sum_ln2_shift,
        sum_w_fc,
        sum_b_fc,
        sum_w_proj,
        sum_b_proj,
    ) = totals
    part_qkv, part_out, part_fc, part_proj = (
        lax.psum_scatter(
            sum_w_qkv.astype(jnp.bfloat16), "seq", scatter_dimension=1, tiled=True
        ).astype(jnp.float32),
        lax.psum_scatter(
            sum_w_out.astype(jnp.bfloat16), "seq", scatter_dimension=1, tiled=True
        ).astype(jnp.float32),
        lax.psum_scatter(
            sum_w_fc.astype(jnp.bfloat16), "seq", scatter_dimension=0, tiled=True
        ).astype(jnp.float32),
        lax.psum_scatter(
            sum_w_proj.astype(jnp.bfloat16), "seq", scatter_dimension=1, tiled=True
        ).astype(jnp.float32),
    )
    bias_qv = lax.dynamic_update_slice_in_dim(
        jnp.zeros((2, feature_width), jnp.float32), sum_b_qv, tensor_index * heads_width, 1
    )
    units_local = sum_b_fc.shape[0]
    bias_fc = lax.dynamic_update_slice_in_dim(
        jnp.zeros((units_local * tensor_count,), jnp.float32),
        sum_b_fc,
        tensor_index * units_local,
        0,
    )
    small_sums = lax.psum(
        (
            sum_ln1_gain,
            sum_ln1_shift,
            bias_qv,
            sum_b_out,
            sum_ln2_gain,
            sum_ln2_shift,
            bias_fc,
            sum_b_proj,
        ),
        ("seq", "tensor"),
    )
    return (
        outputs[None],
        in_grads[None],
        small_sums[0][None],
        small_sums[1][None],
        part_qkv[None],
        small_sums[2][None],
        part_out[None],
        small_sums[3][None],
        small_sums[4][None],
        small_sums[5][None],
        part_fc[None],
        small_sums[6][None],
        part_proj[None],
        small_sums[7][None],
    )


STREAMS = 4
NRM, NMLP, UPS, BRN, ACT, GPRE, MIX, DQKV = range(8)
F32 = jnp.float32
LOW = jnp.bfloat16
MESH_ID = pl.DeviceIdType.MESH


def dot_nn(left, right):
    return lax.dot_general(left, right, (((1,), (0,)), ((), ())), preferred_element_type=F32)


def dot_nt(left, right):
    return lax.dot_general(left, right, (((1,), (1,)), ((), ())), preferred_element_type=F32)


def dot_tn(left, right):
    return lax.dot_general(left, right, (((0,), (0,)), ((), ())), preferred_element_type=F32)


def standard(rows):
    centred = rows - jnp.mean(rows, axis=-1, keepdims=True)
    scale = lax.rsqrt(jnp.mean(centred * centred, axis=-1, keepdims=True) + NORM_EPS)
    return centred * scale, scale


def standard_back(grad, xhat, scale):
    inner = jnp.mean(grad * xhat, axis=-1, keepdims=True)
    return scale * (grad - jnp.mean(grad, axis=-1, keepdims=True) - xhat * inner)


def column_sum(rows):
    return jnp.sum(rows.astype(F32), axis=0, keepdims=True)


def relay_kernel(names, *refs):
    r = types.SimpleNamespace(**dict(zip(names, refs)))
    a, c, t = (lax.axis_index(name) for name in ("section", "seq", "tensor"))
    lines = lax.axis_size("section")
    chips = lax.axis_size("tensor")
    rows, buckets, width = r.inputs.shape[1:]
    half_width = width // 2
    local = rows * chips
    total = 2 * local
    stream_rows = local // STREAMS
    head_width = r.wo_in.shape[0]
    heads = head_width // HDIM
    blocks = local // QB
    units = r.wp_in.shape[0]
    scale = HDIM ** (-0.5)
    streams = range(STREAMS)

    def remote(src, dst, send, recv, **target):
        return pltpu.make_async_remote_copy(
            src_ref=src,
            dst_ref=dst,
            send_sem=send,
            recv_sem=recv,
            device_id=target,
            device_id_type=MESH_ID,
        )

    def drain(ref, sem):
        pltpu.make_async_copy(ref, ref, sem).wait()

    def row_block(index, size):
        return pl.ds(pl.multiple_of(index * size, size), size)

    near_chip = t + 1 - 2 * (t % 2)
    over_chip = (t + 2) % 4
    across_chip = 3 - t
    middle_chip = (t == 1) | (t == 2)
    end_chip = (t == 0) | (t == 3)
    owned = stream_rows // 2
    mine = row_block(t - 1, owned)
    my_half = row_block(c, local)

    barrier = pltpu.get_barrier_semaphore()
    for core in range(2):
        for step in range(1, chips):
            there = {"tensor": (t + step) % chips, "seq": core}
            pl.semaphore_signal(barrier, inc=1, device_id=there, device_id_type=MESH_ID)
        for step in range(1, lines):
            there = {"section": (a + step) % lines, "seq": core}
            pl.semaphore_signal(barrier, inc=1, device_id=there, device_id_type=MESH_ID)
    for step in range(1, lines):
        there = {"section": (a + step) % lines, "tensor": near_chip}
        pl.semaphore_signal(barrier, inc=1, device_id=there, device_id_type=MESH_ID)
    pl.semaphore_signal(barrier, inc=1, device_id={"seq": 1 - c}, device_id_type=MESH_ID)
    pl.semaphore_wait(barrier, 2 * (chips - 1) + 3 * (lines - 1) + 1)

    def beside(s):
        return s + 1 - 2 * (s % 2)

    def above(s):
        return (s + 2) % 4

    def store(p):
        return (r.wq, r.wo, r.wf, r.wp)[p]

    def source(p):
        return (r.wq_in, r.wo_in, r.wf_in, r.wp_in)[p]

    def height(p):
        return source(p).shape[0]

    def core_half(p, s, core):
        return store(p).at[s, row_block(core, height(p) // 2)]

    def first_hop(p, s, neighbour, which):
        return remote(
            source(p).at[row_block(c, height(p) // 2)],
            core_half(p, s, c),
            r.w_first_s.at[p, which],
            r.w_first_r.at[s, p],
            section=neighbour,
        )

    def second_hop(p, s, which):
        view = store(p).at[s, row_block(2 * c + which, height(p) // 4)]
        return remote(
            view, view, r.w_second_s.at[s, p], r.w_second_r.at[s, p, which], section=3 - s
        )

    def core_hop(p, s, core):
        view = core_half(p, s, core)
        return remote(view, view, r.w_core_s.at[s, p], r.w_core_r.at[s, p], seq=1 - c)

    def own_copy(p):
        return pltpu.make_async_copy(source(p), store(p).at[a], r.w_own.at[p])

    def pass_on(s, p, which):
        line = (beside(s), above(s))[which]

        @pl.when(a == line)
        def _():
            first_hop(p, s, line, which).wait_recv()
            second_hop(p, s, which).start()
            core_hop(p, s, c).start()

    def pass_later(pieces):
        for later in range(1, lines):
            for which in range(2):
                if (beside(later), above(later))[which] != 0:
                    for p in pieces:
                        pass_on(later, p, which)

    def pass_far(s, p):
        @pl.when(a == 3 - s)
        def _():
            second_hop(p, s, 0).wait_recv()
            second_hop(p, s, 1).wait_recv()
            core_hop(p, s, c).start()

    def need(s, p):
        @pl.when(s == 0)
        def _():
            pass_on(0, p, 0)
            pass_on(0, p, 1)
            pass_far(0, p)

        @pl.when(a == s)
        def _():
            own_copy(p).wait()

        @pl.when(a != s)
        def _():
            core_hop(p, s, 1 - c).wait_recv()

    def small_copy(step, line, slot):
        return remote(
            r.small_own, r.small.at[slot], r.small_s.at[step], r.small_r.at[slot], section=line
        )

    def count_copy(step, line, slot):
        return remote(
            r.count_own.at[line],
            r.count.at[slot],
            r.count_s.at[step],
            r.count_r.at[slot],
            section=line,
        )

    singles = (r.ln1_gain, r.ln1_shift, r.ln2_gain, r.ln2_shift, r.b_out, r.b_proj)
    for place, single in enumerate(singles):
        r.small_own[place : place + 1] = single[...]
    r.small_own[6:7, :units] = r.b_fc[...]
    r.small_own[7:8, :head_width] = r.b_qv[0:1]
    r.small_own[7:8, half_width : half_width + head_width] = r.b_qv[1:2]
    for step in range(1, lines):
        small_copy(step - 1, (a + step) % lines, a).start()
    for p in range(4):
        for which, line in enumerate((beside(a), above(a))):
            first_hop(p, a, line, which).start()
    for p in range(4):
        own_copy(p).start()
    r.small[a] = r.small_own[...]

    def place_of(index):
        inside = index % local
        stream, left = inside // stream_rows, inside % stream_rows
        first = (index // local) * local + (left // owned) * (local // 2)
        return first + stream * owned + left % owned

    def iota(shape, dimension):
        return lax.broadcasted_iota(jnp.int32, shape, dimension)

    square = jnp.where(iota((KSEL, KSEL), 0) == iota((KSEL, KSEL), 1), 1.0, 0.0).astype(LOW)
    position = place_of(iota((KSEL, total), 1)).astype(F32)
    for pair in range(lines * heads):
        line, head = pair // heads, pair % heads
        columns = dot_nt(square, r.chosen[pair].astype(F32).astype(LOW))
        for block in range(blocks):
            pick = head * blocks + block
            r.count_own[line, pick : pick + 1, :] = jnp.sum(
                jnp.where(columns[:, block : block + 1] == position, 1.0, 0.0),
                axis=0,
                keepdims=True,
            )
    for step in range(1, lines):
        count_copy(step - 1, (a + step) % lines, a).start()
    r.count[a] = r.count_own[a]

    NEAR, OVER, ACROSS = range(3)

    def gather(buffer, s, kind, j, owner, target, slot):
        view = buffer.at[s, j, row_block(owner - 1, owned)]
        return remote(
            view, view, r.ag_s.at[kind, j, slot], r.ag_r.at[kind, j, slot], tensor=target
        )

    def gather_start(buffer, s, kind, j):
        gather(buffer, s, kind, j, t, over_chip, OVER).start()
        gather(buffer, s, kind, j, t, across_chip, ACROSS).start()
        gather(buffer, s, kind, j, t, near_chip, NEAR).start()

    def gather_wait(buffer, s, kind, j):
        @pl.when(middle_chip)
        def _():
            gather(buffer, s, kind, j, across_chip, across_chip, ACROSS).wait_recv()

        @pl.when(end_chip)
        def _():
            gather(buffer, s, kind, j, near_chip, near_chip, NEAR).wait_recv()
            gather(buffer, s, kind, j, over_chip, over_chip, OVER).wait_recv()

    def gather_sent(buffer, s, kind, j):
        @pl.when(middle_chip)
        def _():
            gather(buffer, s, kind, j, t, over_chip, OVER).wait_send()
            gather(buffer, s, kind, j, t, across_chip, ACROSS).wait_send()
            gather(buffer, s, kind, j, t, near_chip, NEAR).wait_send()

    def scatter(s, kind, j, owner, slot):
        return remote(
            r.part.at[kind, j, row_block(owner - 1, owned)],
            r.arrived.at[s, kind, j, slot],
            r.rs_s.at[kind, j, slot],
            r.rs_r.at[kind, j, slot],
            tensor=owner,
        )

    def scatter_start(s, kind, j, product):
        r.part[kind, j] = product.astype(LOW)

        @pl.when(end_chip)
        def _():
            scatter(s, kind, j, over_chip, OVER).start()
            scatter(s, kind, j, near_chip, NEAR).start()

        @pl.when(middle_chip)
        def _():
            scatter(s, kind, j, across_chip, ACROSS).start()

    def scatter_sum(s, kind, j):
        result = r.part[kind, j, mine].astype(F32)
        for slot in (NEAR, ACROSS, OVER):
            scatter(s, kind, j, t, slot).wait_recv()
            result = result + r.arrived[s, kind, j, slot].astype(F32)
        return result

    def scatter_sent(s, kind, j):
        @pl.when(end_chip)
        def _():
            scatter(s, kind, j, over_chip, OVER).wait_send()
            scatter(s, kind, j, near_chip, NEAR).wait_send()

        @pl.when(middle_chip)
        def _():
            scatter(s, kind, j, across_chip, ACROSS).wait_send()

    own_rows = (r.nrm, r.nmlp, r.ups, r.brn, r.act, r.gpre, r.mix, r.dqkv)
    all_rows = (
        r.all_nrm,
        r.all_nmlp,
        r.all_ups,
        r.all_brn,
        r.all_act,
        r.all_gpre,
        r.all_mix,
        r.all_dqkv,
    )

    def rows_copy(index, s, same, stays=False):
        core = c if same else 1 - c
        src = own_rows[index].at[s]
        dst = all_rows[index].at[a, c]
        if index <= BRN:
            src = src.at[:, :, row_block(core, half_width)]
        recv = r.rows_r.at[index]
        if stays:
            return pltpu.make_async_copy(src, dst, recv)
        if same:
            return remote(src, dst, r.rows_s.at[index, s, 0], recv, section=s)
        return remote(src, dst, r.rows_s.at[index, s, 1], recv, section=s, seq=1 - c)

    def rows_start(index, s):
        @pl.when(a == s)
        def _():
            rows_copy(index, s, True, True).start()

        @pl.when(a != s)
        def _():
            rows_copy(index, s, True).start()

        if index <= BRN:
            rows_copy(index, s, False).start()

    def forward_rows(s):
        for index in (NRM, MIX, NMLP, ACT):
            rows_start(index, s)

    def rows_sent(index, s):
        @pl.when(a != s)
        def _():
            rows_copy(index, s, True).wait_send()

        if index <= BRN:
            rows_copy(index, s, False).wait_send()

    def share_copy(index, core):
        view = all_rows[index].at[:, core]
        return remote(view, view, r.share_s.at[index - ACT], r.share_r.at[index - ACT], seq=1 - c)

    def share(index):
        drain(all_rows[index].at[:, c], r.rows_r.at[index])
        share_copy(index, c).start()

    def norm_copy(s):
        return remote(
            r.norm_part.at[s], r.norm_all.at[a], r.norm_s.at[s], r.norm_r, section=s
        )

    def norm_start(s):
        @pl.when(a == s)
        def _():
            pltpu.make_async_copy(r.norm_part.at[s], r.norm_all.at[a], r.norm_r).start()

        @pl.when(a != s)
        def _():
            norm_copy(s).start()

    def home_copy(what, s, chip):
        src, dst, send, recv = what
        return remote(
            src.at[s, chip % 2],
            dst.at[a],
            send.at[s, chip % 2],
            recv,
            section=s,
            tensor=chip,
        )

    def home_start(what, s):
        src, dst, send, recv = what

        @pl.when(middle_chip & (a == s))
        def _():
            pltpu.make_async_copy(src.at[s, t % 2], dst.at[a], recv).start()

        @pl.when(middle_chip & (a != s))
        def _():
            home_copy(what, s, t).start()

        @pl.when(middle_chip)
        def _():
            home_copy(what, s, near_chip).start()

    def home_sent(what, s):
        @pl.when(middle_chip & (a != s))
        def _():
            home_copy(what, s, t).wait_send()

        @pl.when(middle_chip)
        def _():
            home_copy(what, s, near_chip).wait_send()

    out_home = (r.out_low, r.acts, r.out_s, r.out_r)
    grad_home = (r.grad_low, r.grads, r.grad_s, r.grad_r)

    length = r.lengths[a // buckets, a % buckets]
    key = place_of(iota((stream_rows, total), 1))
    for j in streams:
        query = place_of(c * local + j * stream_rows + iota((stream_rows, total), 0))
        r.near[j] = jnp.where((query >= key) & (query - key < WIN), 1.0, 0.0)
    key_row = place_of(iota((1, total), 1))

    def row_mask(place):
        return jnp.where(place < length, 1.0, 0.0)

    def multiplicity(s, j, head):
        far = []
        for block in range(blocks):
            pick = head * blocks + block
            limit = (c * blocks + block) * QB - WIN
            counted = jnp.where(key_row <= limit, r.count[s, pick : pick + 1, :], 0.0)
            far.append(jnp.broadcast_to(counted, (stream_rows // blocks, total)))
        return r.near[j] + jnp.concatenate(far, axis=0)

    def head_cols(head):
        return slice(head * HDIM, (head + 1) * HDIM)

    def kv_copy(s):
        view = r.kv.at[s, :, 0:local]
        return remote(view, view, r.kv_s.at[s], r.kv_r.at[s], seq=1 - c)

    def dkv_copy(s):
        return remote(r.dkv_out.at[s], r.dkv_in.at[s], r.dkv_s.at[s], r.dkv_r.at[s], seq=1 - c)

    def own_sequence(ref):
        both = ref[a // buckets].astype(F32)
        picked = both[:, 0, :]
        for bucket in range(1, buckets):
            picked = jnp.where(a % buckets == bucket, both[:, bucket, :], picked)
        return picked

    def own_part(j):
        chip, first = (j * owned) // rows, (j * owned) % rows
        return chip, slice(first, first + owned)

    def first_copy():
        return remote(r.first_out, r.first_in, r.first_s, r.first_r, tensor=near_chip)

    own_place = c * local + t * rows + iota((rows, 1), 0)
    r.first_out[0] = own_sequence(r.inputs).astype(LOW)
    r.first_out[1] = (own_sequence(r.cotangent) * row_mask(own_place)).astype(LOW)
    r.norm_part[...] = jnp.zeros_like(r.norm_part)

    @pl.when(c == 0)
    def _():
        r.kv[:, :, local:total] = jnp.zeros((lines, 2, local, head_width), LOW)


    @pl.when(end_chip)
    def _():
        first_copy().start()

    @pl.when(middle_chip)
    def _():
        first_copy().wait_recv()
        for which in range(2):
            here, beside_it = r.first_out[which].astype(F32), r.first_in[which].astype(F32)
            lower = jnp.where(t % 2 == 0, here, beside_it)
            upper = jnp.where(t % 2 == 0, beside_it, here)
            for j in streams:
                chip, part = own_part(j)
                own_block = (lower, upper)[chip][part]
                if which == 0:
                    r.hidden[j] = own_block
                else:
                    r.upstream[j] = own_block.astype(LOW)

    def on_owner(stage):
        def run(s, j):
            @pl.when(middle_chip)
            def _():
                stage(s, j)

        return run

    def keep_rows(target, s, j, result):
        chip, part = own_part(j)
        target[s, chip, part] = result

    @on_owner
    def enter(s, j):
        xhat, inverse = standard(r.hidden[j])
        r.xhat1[s, j] = xhat
        r.inv1[s, j] = jnp.broadcast_to(inverse, (owned, 128))
        r.nrm[s, j, mine] = (xhat * r.small[s, 0:1] + r.small[s, 1:2]).astype(LOW)
        gather_start(r.nrm, s, 0, j)

    def project(s, j):
        gather_wait(r.nrm, s, 0, j)
        normed = r.nrm[s, j]
        place = row_block(c * STREAMS + j, stream_rows)
        bias_v = r.small[s, 7:8, half_width : half_width + head_width]
        key_rows = dot_nt(normed, r.wq[s, head_width : 2 * head_width])
        value_rows = dot_nt(normed, r.wq[s, 2 * head_width : 3 * head_width]) + bias_v
        r.kv[s, 0, place] = key_rows.astype(LOW)
        r.kv[s, 1, place] = value_rows.astype(LOW)
        gather_sent(r.nrm, s, 0, j)

    def ask(s, j):
        queries = dot_nt(r.nrm[s, j], r.wq[s, 0:head_width]) + r.small[s, 7:8, :head_width]
        r.qry[s, j] = queries.astype(LOW)

    def attend_line(s, j):
        mixed = []
        for head in range(heads):
            cols = head_cols(head)
            times = multiplicity(s, j, head)
            scores = scale * dot_nt(r.qry[s, j, :, cols], r.kv[s, 0, :, cols])
            scores = jnp.where(times > 0.0, scores, MASKED)
            top = jnp.max(scores, axis=-1, keepdims=True)
            terms = times * jnp.exp(scores - top)
            weights = terms / jnp.sum(terms, axis=-1, keepdims=True)
            r.soft[s, j, head] = weights
            mixed.append(dot_nn(weights.astype(LOW), r.kv[s, 1, :, cols]))
        mask = row_mask(place_of(c * local + j * stream_rows + iota((stream_rows, 1), 0)))
        r.mix[s, j] = (jnp.concatenate(mixed, axis=-1) * mask).astype(LOW)

    def leave_attention(s, j):
        scatter_start(s, 0, j, dot_nn(r.mix[s, j], r.wo[s]))

    @on_owner
    def between(s, j):
        middle = r.hidden[j] + scatter_sum(s, 0, j) + r.small[s, 4:5]
        r.middle[j] = middle
        xhat, inverse = standard(middle)
        r.xhat2[s, j] = xhat
        r.inv2[s, j] = jnp.broadcast_to(inverse, (owned, 128))
        r.nmlp[s, j, mine] = (xhat * r.small[s, 2:3] + r.small[s, 3:4]).astype(LOW)
        gather_start(r.nmlp, s, 1, j)

    def feed(s, j):
        gather_wait(r.nmlp, s, 1, j)
        before = dot_nn(r.nmlp[s, j], r.wf[s]) + r.small[s, 6:7, :units]
        bend = jnp.tanh(0.7978845608028654 * (before + 0.044715 * before * before * before))
        r.act[s, j] = (0.5 * before * (1.0 + bend)).astype(LOW)
        r.slope[s, j] = 0.5 * (1.0 + bend) + 0.5 * before * (1.0 - bend * bend) * (
            0.7978845608028654 * (1.0 + 3 * 0.044715 * before * before)
        )

        gather_sent(r.nmlp, s, 1, j)

    def leave_feed(s, j):
        scatter_start(s, 1, j, dot_nn(r.act[s, j], r.wp[s]))

    @on_owner
    def finish(s, j):
        result = r.middle[j] + scatter_sum(s, 1, j) + r.small[s, 5:6]
        keep_rows(r.out_low, s, j, result.astype(LOW))
        r.hidden[j] = result.astype(LOW).astype(F32)

    def small_ready(s):
        @pl.when(a != s)
        def _():
            small_copy(0, a, s).wait_recv()

    small_ready(0)
    for j in streams:
        enter(0, j)

    def forward(s, _):
        need(s, 0)
        for j in streams:
            project(s, j)

        @pl.when(c == 0)
        def _():
            kv_copy(s).start()

        for j in streams:
            ask(s, j)

        @pl.when(a != s)
        def _():
            count_copy(0, a, s).wait_recv()

        @pl.when(c == 1)
        def _():
            kv_copy(s).wait_recv()

        for j in streams:
            attend_line(s, j)
            if j == 0:
                need(s, 1)
            leave_attention(s, j)

        @pl.when(s == 0)
        def _():
            pass_later((0, 1))

        @pl.when(s == 1)
        def _():
            pass_on(1, 2, 0)
            pass_on(1, 3, 0)
            for p in range(4):
                pass_on(2, p, 1)

        @pl.when(s > 0)
        def _():
            pass_far(s, 2)
            pass_far(s, 3)

        for j in streams:
            between(s, j)
            scatter_sent(s, 0, j)
        need(s, 2)

        @pl.when(s == 0)
        def _():
            pass_later((2,))

        for j in streams:
            feed(s, j)
            if j == 0:
                need(s, 3)
            leave_feed(s, j)

        @pl.when(s == 0)
        def _():
            pass_later((3,))


        @pl.when(s >= 2)
        def _():
            forward_rows(s - 2)


        @pl.when(s + 1 < lines)
        def _():
            small_ready(s + 1)

        for j in streams:
            finish(s, j)
            scatter_sent(s, 1, j)

            @pl.when(s + 1 < lines)
            def _():
                enter(s + 1, j)

        home_start(out_home, s)

        @pl.when(s == 0)
        def _():
            pass_on(1, 0, 0)
            pass_on(1, 1, 0)

        @pl.when(s + 1 < lines)
        def _():
            pass_far(s + 1, 0)
            pass_far(s + 1, 1)

        return 0

    lax.fori_loop(0, lines, forward, 0)

    @on_owner
    def turn(s, j):
        upstream = r.upstream[j]
        r.ups[s, j, mine] = upstream
        gather_start(r.ups, s, 2, j)
        r.norm_part[s, 5:6] += column_sum(upstream)

    def feed_back(s, j):
        gather_wait(r.ups, s, 2, j)
        grad_pre = (dot_nt(r.ups[s, j], r.wp[s]) * r.slope[s, j]).astype(LOW)
        r.gpre[s, j] = grad_pre
        scatter_start(s, 2, j, dot_nt(grad_pre, r.wf[s]))
        r.norm_part[s, 6:7, :units] += column_sum(grad_pre)
        gather_sent(r.ups, s, 2, j)

    @on_owner
    def between_back(s, j):
        grad = scatter_sum(s, 2, j)
        xhat = r.xhat2[s, j]
        upstream = r.upstream[j].astype(F32)
        grad_middle = upstream + standard_back(
            grad * r.small[s, 2:3], xhat, r.inv2[s, j, :, 0:1]
        )
        r.middle[j] = grad_middle
        branch = grad_middle.astype(LOW)
        r.brn[s, j, mine] = branch
        gather_start(r.brn, s, 3, j)
        r.norm_part[s, 2:3] += column_sum(grad * xhat)
        r.norm_part[s, 3:4] += column_sum(grad)
        r.norm_part[s, 4:5] += column_sum(branch)

    def mixed_back(s, j):
        gather_wait(r.brn, s, 3, j)
        place = place_of(c * local + j * stream_rows + iota((stream_rows, 1), 0))
        r.gmix[j] = (dot_nt(r.brn[s, j], r.wo[s]) * row_mask(place)).astype(LOW)
        gather_sent(r.brn, s, 3, j)

    def attend_line_back(s, j):
        grad_q, grad_k, grad_v = [], [], []
        for head in range(heads):
            cols = head_cols(head)
            weights = r.soft[s, j, head]
            grad_head = r.gmix[j, :, cols]
            grad_weights = dot_nt(grad_head, r.kv[s, 1, :, cols])
            inner = jnp.sum(weights * grad_weights, axis=-1, keepdims=True)
            grad_scores = (weights * (grad_weights - inner)).astype(LOW)
            grad_k.append(scale * dot_tn(grad_scores, r.qry[s, j, :, cols]))
            grad_v.append(dot_tn(weights.astype(LOW), grad_head))
            grad_q.append(scale * dot_nn(grad_scores, r.kv[s, 0, :, cols]))
        for which, grad in enumerate((grad_k, grad_v)):
            grad = jnp.concatenate(grad, axis=-1)
            r.dkv_all[which] = grad if j == 0 else r.dkv_all[which] + grad
        grad_q = jnp.concatenate(grad_q, axis=-1).astype(LOW)
        r.dqkv[s, 0, j] = grad_q
        r.norm_part[s, 7:8, :head_width] += column_sum(grad_q)

    def join_keys(s):
        @pl.when(c == 1)
        def _():
            r.dkv_out[s] = r.dkv_all[:, 0:local].astype(LOW)
            dkv_copy(s).start()

        @pl.when(c == 0)
        def _():
            dkv_copy(s).wait_recv()
            r.dkv_all[:, 0:local] += r.dkv_in[s].astype(F32)

        for which in range(2):
            joined = r.dkv_all[which, my_half].astype(LOW)
            r.dqkv[s, 1 + which] = joined.reshape(r.dqkv.shape[2:])
            if which == 1:
                r.norm_part[s, 7:8, half_width : half_width + head_width] = column_sum(joined)

    def leave_back(s, j):
        product = dot_nn(r.dqkv[s, 0, j], r.wq[s, 0:head_width])
        for which in range(1, 3):
            weight = r.wq[s, which * head_width : (which + 1) * head_width]
            product = product + dot_nn(r.dqkv[s, which, j], weight)
        scatter_start(s, 3, j, product)

    @on_owner
    def finish_back(s, j):
        grad = scatter_sum(s, 3, j)
        xhat = r.xhat1[s, j]
        result = r.middle[j] + standard_back(
            grad * r.small[s, 0:1], xhat, r.inv1[s, j, :, 0:1]
        )
        r.upstream[j] = result.astype(LOW)
        keep_rows(r.grad_low, s, j, result.astype(LOW))
        r.norm_part[s, 0:1] += column_sum(grad * xhat)
        r.norm_part[s, 1:2] += column_sum(grad)

    for j in streams:
        turn(lines - 1, j)

    def backward(index, _):
        s = lines - 1 - index
        for j in streams:
            feed_back(s, j)
        rows_start(UPS, s)
        rows_start(GPRE, s)

        @pl.when(index < 2)
        def _():
            forward_rows(lines - 2 + index)

        @pl.when(index == lines - 1)
        def _():
            share(ACT)
            share(MIX)

        for j in streams:
            between_back(s, j)
            scatter_sent(s, 2, j)
        for j in streams:
            mixed_back(s, j)
            attend_line_back(s, j)
        join_keys(s)
        rows_start(BRN, s)
        for j in streams:
            leave_back(s, j)
        rows_start(DQKV, s)
        for j in streams:
            finish_back(s, j)
            scatter_sent(s, 3, j)

            @pl.when(s > 0)
            def _():
                turn(s - 1, j)

        norm_start(s)
        home_start(grad_home, s)
        return 0

    lax.fori_loop(0, lines, backward, 0)

    share(GPRE)
    share(DQKV)

    drain(r.norm_all, r.norm_r)
    slot = c * chips + t
    norm_sum = r.norm_all[0]
    for line in range(1, lines):
        norm_sum = norm_sum + r.norm_all[line]
    r.ends[slot] = norm_sum

    def ends_copy(step):
        core, chip = step // chips, step % chips
        view = r.ends.at[slot]
        return remote(
            view,
            view,
            r.ends_s.at[step - 1],
            r.ends_r,
            seq=(c + core) % 2,
            tensor=(t + chip) % chips,
        )

    for step in range(1, 2 * chips):
        ends_copy(step).start()

    for index in range(ACT):
        drain(all_rows[index], r.rows_r.at[index])
    for index in range(ACT, 8):
        share_copy(index, 1 - c).wait_recv()
        share_copy(index, c).wait_send()
    drain(r.acts, r.out_r)
    drain(r.grads, r.grad_r)
    drain(r.ends.at[0 : 2 * chips - 1], r.ends_r)
    for step in range(1, 2 * chips):
        ends_copy(step).wait_send()
    for step in range(1, lines):
        small_copy(step - 1, (a + step) % lines, a).wait_send()
        count_copy(step - 1, (a + step) % lines, a).wait_send()
    for p in range(4):
        for which, line in enumerate((beside(a), above(a))):
            first_hop(p, a, line, which).wait_send()

    @pl.when(end_chip)
    def _():
        first_copy().wait_send()

    def sent(s, _):
        home_sent(out_home, s)
        home_sent(grad_home, s)

        @pl.when(a != s)
        def _():
            norm_copy(s).wait_send()

        @pl.when(c == 0)
        def _():
            kv_copy(s).wait_send()

        @pl.when(c == 1)
        def _():
            dkv_copy(s).wait_send()

        for index in range(8):
            rows_sent(index, s)
        for p in range(4):

            @pl.when((a == beside(s)) | (a == above(s)))
            def _():
                second_hop(p, s, 0).wait_send()

            @pl.when(a != s)
            def _():
                core_hop(p, s, c).wait_send()

        return 0

    lax.fori_loop(0, lines, sent, 0)


def relay_call(inputs, cotangent, lengths, chosen, singles, weights):
    lines = lax.axis_size("section")
    chips = lax.axis_size("tensor")
    rows, buckets, width = inputs.shape[1:]
    local, total, half = rows * chips, 2 * rows * chips, width // 2
    head_width, units = weights["wo_in"].shape[0], weights["wp_in"].shape[0]
    heads = head_width // HDIM
    stream = local // STREAMS
    peers, owned = chips - 1, stream // 2
    vmem, dma = pltpu.VMEM, pltpu.SemaphoreType.DMA
    operands = dict(
        inputs=inputs,
        cotangent=cotangent,
        lengths=lengths,
        chosen=chosen,
        **singles,
        **weights,
    )

    def space(name):
        if name in weights:
            return pl.ANY
        return pltpu.SMEM if operands[name] is lengths else pltpu.VMEM

    sums = dict(
        acts=((lines, rows, width), LOW),
        grads=((lines, rows, width), LOW),
        ends=((2 * chips, 8, width), F32),
    )
    gathered = dict(
        all_nrm=((lines, 2, STREAMS, stream, half), LOW),
        all_nmlp=((lines, 2, STREAMS, stream, half), LOW),
        all_ups=((lines, 2, STREAMS, stream, half), LOW),
        all_brn=((lines, 2, STREAMS, stream, half), LOW),
        all_act=((lines, 2, STREAMS, stream, units), LOW),
        all_gpre=((lines, 2, STREAMS, stream, units), LOW),
        all_mix=((lines, 2, STREAMS, stream, head_width), LOW),
        all_dqkv=((lines, 2, 3, STREAMS, stream, head_width), LOW),
    )
    outputs = dict(**sums, **gathered)
    scratch = dict(
        wq=vmem((lines,) + weights["wq_in"].shape, LOW),
        wo=vmem((lines,) + weights["wo_in"].shape, LOW),
        wf=vmem((lines,) + weights["wf_in"].shape, LOW),
        wp=vmem((lines,) + weights["wp_in"].shape, LOW),
        small_own=vmem((8, width), F32),
        small=vmem((lines, 8, width), F32),
        count_own=vmem((lines, 8, total), F32),
        count=vmem((lines, 8, total), F32),
        hidden=vmem((STREAMS, owned, width), F32),
        middle=vmem((STREAMS, owned, width), F32),
        upstream=vmem((STREAMS, owned, width), LOW),
        first_out=vmem((2, rows, width), LOW),
        first_in=vmem((2, rows, width), LOW),
        xhat1=vmem((lines, STREAMS, owned, width), F32),
        inv1=vmem((lines, STREAMS, owned, 128), F32),
        xhat2=vmem((lines, STREAMS, owned, width), F32),
        inv2=vmem((lines, STREAMS, owned, 128), F32),
        nrm=vmem((lines, STREAMS, stream, width), LOW),
        nmlp=vmem((lines, STREAMS, stream, width), LOW),
        ups=vmem((lines, STREAMS, stream, width), LOW),
        brn=vmem((lines, STREAMS, stream, width), LOW),
        act=vmem((lines, STREAMS, stream, units), LOW),
        gpre=vmem((lines, STREAMS, stream, units), LOW),
        slope=vmem((lines, STREAMS, stream, units), F32),
        mix=vmem((lines, STREAMS, stream, head_width), LOW),
        qry=vmem((lines, STREAMS, stream, head_width), LOW),
        gmix=vmem((STREAMS, stream, head_width), LOW),
        dqkv=vmem((lines, 3, STREAMS, stream, head_width), LOW),
        kv=vmem((lines, 2, total, head_width), LOW),
        soft=vmem((lines, STREAMS, heads, stream, total), F32),
        near=vmem((STREAMS, stream, total), F32),
        dkv_all=vmem((2, total, head_width), F32),
        dkv_out=vmem((lines, 2, local, head_width), LOW),
        dkv_in=vmem((lines, 2, local, head_width), LOW),
        part=vmem((4, STREAMS, stream, width), LOW),
        arrived=vmem((lines, 4, STREAMS, peers, owned, width), LOW),
        out_low=vmem((lines, 2, rows, width), LOW),
        grad_low=vmem((lines, 2, rows, width), LOW),
        norm_part=vmem((lines, 8, width), F32),
        norm_all=vmem((lines, 8, width), F32),
        w_first_s=dma((4, 2)),
        w_first_r=dma((lines, 4)),
        w_second_s=dma((lines, 4)),
        w_second_r=dma((lines, 4, 2)),
        w_core_s=dma((lines, 4)),
        w_core_r=dma((lines, 4)),
        w_own=dma((4,)),
        small_s=dma((lines - 1,)),
        small_r=dma((lines,)),
        count_s=dma((lines - 1,)),
        count_r=dma((lines,)),
        ag_s=dma((4, STREAMS, peers)),
        ag_r=dma((4, STREAMS, peers)),
        rs_s=dma((4, STREAMS, peers)),
        rs_r=dma((4, STREAMS, peers)),
        kv_s=dma((lines,)),
        kv_r=dma((lines,)),
        dkv_s=dma((lines,)),
        dkv_r=dma((lines,)),
        rows_s=dma((8, lines, 2)),
        rows_r=dma((8,)),
        share_s=dma((4,)),
        share_r=dma((4,)),
        first_s=dma,
        first_r=dma,
        out_s=dma((lines, 2)),
        out_r=dma,
        grad_s=dma((lines, 2)),
        grad_r=dma,
        norm_s=dma((lines,)),
        norm_r=dma,
        ends_s=dma((2 * chips - 1,)),
        ends_r=dma,
    )
    names = tuple(operands) + tuple(outputs) + tuple(scratch)
    results = pl.pallas_call(
        functools.partial(relay_kernel, names),
        out_shape=[jax.ShapeDtypeStruct(shape, kind) for shape, kind in outputs.values()],
        in_specs=[pl.BlockSpec(memory_space=space(name)) for name in operands],
        out_specs=[
            pl.BlockSpec(memory_space=pl.ANY if name in gathered else pltpu.VMEM)
            for name in outputs
        ],
        scratch_shapes=list(scratch.values()),
        compiler_params=pltpu.CompilerParams(
            collective_id=0, has_side_effects=True, vmem_limit_bytes=60 * 2**20
        ),
        name="relay",
    )(*operands.values())
    return dict(zip(outputs, results))


def weights_kernel(names, *refs):
    r = types.SimpleNamespace(**dict(zip(names, refs)))
    step = pl.program_id(0)
    micro_count, rows, buckets, width = r.activations.shape
    chips, units, head_width = r.ends.shape[0] // 2, r.all_act.shape[-1], r.all_mix.shape[-1]

    @pl.when(step == 0)
    def _():
        sums = r.ends[0]
        for other in range(1, 2 * chips):
            sums = sums + r.ends[other]
        singles = (r.ln1_gain, r.ln1_shift, r.ln2_gain, r.ln2_shift, r.b_out, r.b_proj)
        for place, single in enumerate(singles):
            single[...] = sums[place : place + 1]
        for chip in range(chips):
            both = r.ends[chip] + r.ends[chips + chip]
            r.b_fc[:, chip * units : (chip + 1) * units] = both[6:7, :units]
            here = slice(chip * head_width, (chip + 1) * head_width)
            r.b_qv[0:1, here] = both[7:8, :head_width]
            r.b_qv[1:2, here] = both[7:8, width // 2 : width // 2 + head_width]
        for target, source in ((r.activations, r.acts), (r.in_grads, r.grads)):
            for micro in range(micro_count):
                rows_of = [
                    source[micro * buckets + bucket].astype(F32)[:, None, :]
                    for bucket in range(buckets)
                ]
                target[micro] = jnp.concatenate(rows_of, axis=1).astype(LOW)
        for target in (r.w_qkv, r.w_out, r.w_fc, r.w_proj):
            target[...] = jnp.zeros_like(target)

    def rows_of_sequence(ref):
        return ref[0].reshape(2 * chips * rows, ref.shape[-1])

    nrm, nmlp, ups, brn, act, gpre, mix = (
        rows_of_sequence(ref)
        for ref in (r.all_nrm, r.all_nmlp, r.all_ups, r.all_brn, r.all_act, r.all_gpre, r.all_mix)
    )
    r.w_proj[...] += dot_tn(act, ups)
    r.w_fc[...] += dot_tn(nmlp, gpre)
    r.w_out[...] += dot_tn(mix, brn)
    for which in range(3):
        grad = r.all_dqkv[0, :, which].reshape(2 * chips * rows, head_width)
        r.w_qkv[which] += dot_tn(grad, nrm)


def weights_call(relayed, inputs_shape, head_width, units):
    lines = lax.axis_size("section")
    chips = lax.axis_size("tensor")
    width = inputs_shape[-1]
    half = width // 2
    outputs = dict(
        activations=(inputs_shape, LOW),
        in_grads=(inputs_shape, LOW),
        ln1_gain=((1, width), F32),
        ln1_shift=((1, width), F32),
        w_qkv=((3, head_width, half), F32),
        b_qv=((2, width), F32),
        w_out=((head_width, half), F32),
        b_out=((1, width), F32),
        ln2_gain=((1, width), F32),
        ln2_shift=((1, width), F32),
        w_fc=((half, units), F32),
        b_fc=((1, chips * units), F32),
        w_proj=((units, half), F32),
        b_proj=((1, width), F32),
    )

    def spec(array):
        if len(array.shape) < 5:
            return pl.BlockSpec(array.shape, lambda step: (0,) * len(array.shape))
        return pl.BlockSpec(
            (1,) + array.shape[1:], lambda step: (step,) + (0,) * (len(array.shape) - 1)
        )

    def whole(shape):
        return pl.BlockSpec(shape, lambda step: (0,) * len(shape))

    return pl.pallas_call(
        functools.partial(weights_kernel, tuple(relayed) + tuple(outputs)),
        out_shape=[jax.ShapeDtypeStruct(shape, kind) for shape, kind in outputs.values()],
        grid=(lines,),
        in_specs=[spec(array) for array in relayed.values()],
        out_specs=[whole(shape) for shape, _ in outputs.values()],
        compiler_params=pltpu.CompilerParams(vmem_limit_bytes=60 * 2**20),
        name="weight_gradients",
    )(*relayed.values())


def on_line(
    inputs,
    cotangent,
    lengths,
    chosen,
    ln1_gain,
    ln1_shift,
    w_qkv,
    b_qv,
    w_out,
    b_out,
    ln2_gain,
    ln2_shift,
    w_fc,
    b_fc,
    w_proj,
    b_proj,
):
    head_width, units = w_out.shape[1], w_fc.shape[2]
    singles = dict(
        ln1_gain=ln1_gain,
        ln1_shift=ln1_shift,
        ln2_gain=ln2_gain,
        ln2_shift=ln2_shift,
        b_out=b_out,
        b_proj=b_proj,
        b_fc=b_fc,
        b_qv=b_qv[0],
    )
    weights = dict(
        wq_in=jnp.swapaxes(w_qkv[0], 1, 2).reshape(-1, inputs.shape[-1]),
        wo_in=w_out[0],
        wf_in=w_fc[0],
        wp_in=w_proj[0],
    )
    picks = chosen.reshape((-1,) + chosen.shape[-2:])
    relayed = relay_call(inputs, cotangent, lengths, picks, singles, weights)
    results = list(weights_call(relayed, inputs.shape, head_width, units))
    results[4] = jnp.swapaxes(results[4], 1, 2)
    vectors = (2, 3, 7, 8, 9, 11, 13)
    return tuple(
        result if place in vectors else result[None] for place, result in enumerate(results)
    )


def fits_lines(mesh):
    return mesh.shape["section"] == 4 and mesh.shape["seq"] == 2 and mesh.shape["tensor"] == 4


def solution(mesh):
    placed = (
        P(None, ("seq", "tensor"), None, None),
        P(None, ("seq", "tensor"), None, None),
        P(),
        P("section", None, None, "tensor", "seq", None),
        P("section", None),
        P("section", None),
        P("section", None, None, "tensor"),
        P("section", None, "tensor"),
        P("section", "tensor", None),
        P("section", None),
        P("section", None),
        P("section", None),
        P("section", None, "tensor"),
        P("section", "tensor"),
        P("section", "tensor", None),
        P("section", None),
    )
    return jax.shard_map(
        on_line if fits_lines(mesh) else on_device,
        mesh=mesh,
        in_specs=placed,
        out_specs=(
            P("section", None, ("seq", "tensor"), None, None),
            P("section", None, ("seq", "tensor"), None, None),
            P("section", None),
            P("section", None),
            P("section", None, "seq", "tensor"),
            P("section", None, None),
            P("section", "tensor", "seq"),
            P("section", None),
            P("section", None),
            P("section", None),
            P("section", "seq", "tensor"),
            P("section", None),
            P("section", "tensor", "seq"),
            P("section", None),
        ),
        check_vma=False,
    )
```

```python
import functools
import types

import jax
import jax.numpy as jnp
from jax import lax
from jax.experimental import pallas as pl
from jax.experimental.pallas import tpu as pltpu
from jax.sharding import PartitionSpec as P

HDIM = 64
WIN = 64
QB = 64
KSEL = 64


NORM_EPS = 1e-05
MASKED = -1000000000.0


def from_behind(value, axis, steps):
    count = lax.axis_size(axis)
    first, last = (max(0, -steps), min(count, count - steps))
    return lax.ppermute(value, axis, [(source, source + steps) for source in range(first, last)])


def layer_norm(values, gain, shift):
    average = jnp.mean(values, axis=-1, keepdims=True)
    centred = values - average
    variance = jnp.mean(centred * centred, axis=-1, keepdims=True)
    return centred * lax.rsqrt(variance + NORM_EPS) * gain + shift


def gelu_tanh(values):
    return (
        0.5
        * values
        * (1.0 + jnp.tanh(0.7978845608028654 * (values + 0.044715 * values * values * values)))
    )


def gather_rows(row_block):
    return lax.all_gather(row_block, "tensor", axis=0, tiled=True)


def scatter_product(left_rows, weight, formula):
    return lax.psum_scatter(
        jnp.einsum(formula, left_rows, weight, preferred_element_type=jnp.float32).astype(
            jnp.bfloat16
        ),
        "tensor",
        scatter_dimension=0,
        tiled=True,
    ).astype(jnp.float32)


def near_slabs(full_rows, seq_start, seq_first, length_local):
    buckets = full_rows.shape[1]
    heads_local = full_rows.shape[2] // HDIM
    blocks = length_local // QB
    earlier = lax.dynamic_slice_in_dim(full_rows, jnp.maximum(seq_start - WIN, 0), WIN, 0)
    earlier = jnp.where(seq_first, jnp.zeros_like(earlier), earlier)
    local_part = lax.dynamic_slice_in_dim(full_rows, seq_start, length_local, 0)
    segment = jnp.concatenate([earlier, local_part], 0).reshape(
        length_local + WIN, buckets, heads_local, HDIM
    )
    return jnp.concatenate(
        [
            segment[offset_index * QB : offset_index * QB + length_local].reshape(
                blocks, QB, buckets, heads_local, HDIM
            )
            for offset_index in range(WIN // QB + 1)
        ],
        1,
    )


def far_rows(full_rows, flat_index):
    total_rows, buckets, feature_width = full_rows.shape
    heads_local = feature_width // HDIM
    return jnp.take(full_rows.reshape(total_rows * buckets * heads_local, HDIM), flat_index, axis=0)


def key_geometry(chosen_now, seq_start, blocks):
    buckets, heads_local = (chosen_now.shape[0], chosen_now.shape[1])
    bucket_ids = lax.broadcasted_iota(jnp.int32, chosen_now.shape, 0)
    head_ids = lax.broadcasted_iota(jnp.int32, chosen_now.shape, 1)
    flat_index = (chosen_now * buckets + bucket_ids) * heads_local + head_ids
    block_start = seq_start + QB * lax.broadcasted_iota(jnp.int32, (blocks, 1, 1), 0)
    query_ids = lax.broadcasted_iota(jnp.int32, (1, QB, 1), 1)
    key_ids = lax.broadcasted_iota(jnp.int32, (1, 1, WIN + QB), 2)
    distance = query_ids + WIN - key_ids
    near_ok = (distance >= 0) & (distance < WIN) & (block_start + key_ids - WIN >= 0)
    far_ok = chosen_now + WIN <= block_start.reshape(1, 1, blocks, 1)
    near_mask = jnp.broadcast_to(
        near_ok[:, None, None], (blocks, buckets, heads_local, QB, WIN + QB)
    )
    far_mask = jnp.broadcast_to(
        jnp.transpose(far_ok, (2, 0, 1, 3))[:, :, :, None, :],
        (blocks, buckets, heads_local, QB, KSEL),
    )
    return (flat_index, jnp.concatenate([near_mask, far_mask], -1))


def attention_setup(queries, key_rows, value_rows, chosen_now, seq_start, seq_first):
    length_local, buckets, feature_width = queries.shape
    heads_local = feature_width // HDIM
    blocks = length_local // QB
    query_blocks = queries.reshape(blocks, QB, buckets, heads_local, HDIM)
    flat_index, key_mask = key_geometry(chosen_now, seq_start, blocks)
    near_keys = near_slabs(key_rows, seq_start, seq_first, length_local)
    near_values = near_slabs(value_rows, seq_start, seq_first, length_local)
    far_keys = far_rows(key_rows, flat_index)
    far_values = far_rows(value_rows, flat_index)
    near_scores = jnp.einsum(
        "bqnhe,btnhe->bnhqt", query_blocks, near_keys, preferred_element_type=jnp.float32
    )
    far_scores = jnp.einsum(
        "bqnhe,nhbke->bnhqk", query_blocks, far_keys, preferred_element_type=jnp.float32
    )
    scores = jnp.where(
        key_mask, HDIM ** (-0.5) * jnp.concatenate([near_scores, far_scores], -1), MASKED
    )
    return (query_blocks, near_keys, near_values, far_keys, far_values, flat_index, scores)


def attend(queries, key_rows, value_rows, chosen_now, seq_start, seq_first):
    query_blocks, near_keys, near_values, far_keys, far_values, flat_index, scores = (
        attention_setup(queries, key_rows, value_rows, chosen_now, seq_start, seq_first)
    )
    span = WIN + QB
    row_top = jnp.max(scores, -1, keepdims=True)
    exp_terms = jnp.exp(scores - row_top)
    row_total = jnp.sum(exp_terms, -1, keepdims=True)
    softmax_low = (exp_terms / row_total).astype(jnp.bfloat16)
    near_part = jnp.einsum(
        "bnhqt,btnhe->bqnhe",
        softmax_low[..., :span],
        near_values,
        preferred_element_type=jnp.float32,
    )
    far_part = jnp.einsum(
        "bnhqk,nhbke->bqnhe",
        softmax_low[..., span:],
        far_values,
        preferred_element_type=jnp.float32,
    )
    return ((near_part + far_part).reshape(queries.shape), row_top + jnp.log(row_total))


def spread_back(near_grad, far_grad, flat_index, seq_start, seq_first, total_rows):
    blocks, span, buckets, heads_local, head_size = near_grad.shape
    length_local = blocks * QB
    feature_width = heads_local * head_size
    segment = jnp.zeros((length_local + WIN, buckets, heads_local, head_size), jnp.float32)
    for offset_index in range(WIN // QB + 1):
        piece = near_grad[:, offset_index * QB : (offset_index + 1) * QB].reshape(
            length_local, buckets, heads_local, head_size
        )
        segment = segment.at[offset_index * QB : offset_index * QB + length_local].add(piece)
    full_rows = jnp.zeros((total_rows * buckets * heads_local, head_size), jnp.float32)
    full_rows = full_rows.at[flat_index.reshape(-1)].add(far_grad.reshape(-1, head_size))
    full_rows = full_rows.reshape(total_rows, buckets, feature_width)
    local_part = segment[WIN:].reshape(length_local, buckets, feature_width)
    earlier = jnp.where(seq_first, 0.0, segment[:WIN].reshape(WIN, buckets, feature_width))
    full_rows = lax.dynamic_update_slice_in_dim(
        full_rows,
        lax.dynamic_slice_in_dim(full_rows, seq_start, length_local, 0) + local_part,
        seq_start,
        0,
    )
    earlier_start = jnp.maximum(seq_start - WIN, 0)
    full_rows = lax.dynamic_update_slice_in_dim(
        full_rows,
        lax.dynamic_slice_in_dim(full_rows, earlier_start, WIN, 0) + earlier,
        earlier_start,
        0,
    )
    return full_rows


def attend_back(
    queries, key_rows, value_rows, chosen_now, seq_start, seq_first, log_total, grad_mixed
):
    query_blocks, near_keys, near_values, far_keys, far_values, flat_index, scores = (
        attention_setup(queries, key_rows, value_rows, chosen_now, seq_start, seq_first)
    )
    span = WIN + QB
    score_scale = HDIM ** (-0.5)
    grad_blocks = grad_mixed.reshape(query_blocks.shape)
    weights_full = jnp.exp(scores - log_total)
    softmax_low = weights_full.astype(jnp.bfloat16)
    grad_near_weights = jnp.einsum(
        "bqnhe,btnhe->bnhqt", grad_blocks, near_values, preferred_element_type=jnp.float32
    )
    grad_far_weights = jnp.einsum(
        "bqnhe,nhbke->bnhqk", grad_blocks, far_values, preferred_element_type=jnp.float32
    )
    grad_weights = jnp.concatenate([grad_near_weights, grad_far_weights], -1)
    row_dot = jnp.sum(weights_full * grad_weights, -1, keepdims=True)
    grad_scores = (weights_full * (grad_weights - row_dot)).astype(jnp.bfloat16)
    grad_near, grad_far = (grad_scores[..., :span], grad_scores[..., span:])
    grad_queries = score_scale * (
        jnp.einsum("bnhqt,btnhe->bqnhe", grad_near, near_keys, preferred_element_type=jnp.float32)
        + jnp.einsum("bnhqk,nhbke->bqnhe", grad_far, far_keys, preferred_element_type=jnp.float32)
    )
    near_key_grad = score_scale * jnp.einsum(
        "bnhqt,bqnhe->btnhe", grad_near, query_blocks, preferred_element_type=jnp.float32
    )
    far_key_grad = score_scale * jnp.einsum(
        "bnhqk,bqnhe->nhbke", grad_far, query_blocks, preferred_element_type=jnp.float32
    )
    near_value_grad = jnp.einsum(
        "bnhqt,bqnhe->btnhe",
        softmax_low[..., :span],
        grad_blocks,
        preferred_element_type=jnp.float32,
    )
    far_value_grad = jnp.einsum(
        "bnhqk,bqnhe->nhbke",
        softmax_low[..., span:],
        grad_blocks,
        preferred_element_type=jnp.float32,
    )
    total_rows = key_rows.shape[0]
    key_grad = spread_back(
        near_key_grad, far_key_grad, flat_index, seq_start, seq_first, total_rows
    )
    value_grad = spread_back(
        near_value_grad, far_value_grad, flat_index, seq_start, seq_first, total_rows
    )
    return (grad_queries.reshape(queries.shape), key_grad, value_grad)


def forward_pass(hidden, params, chosen_now, query_mask, seq_start, seq_first, finish):
    (
        ln1_gain,
        ln1_shift,
        w_qkv,
        b_qv,
        w_out,
        b_out,
        ln2_gain,
        ln2_shift,
        w_fc,
        b_fc,
        w_proj,
        b_proj,
    ) = params
    hidden_wide = hidden.astype(jnp.float32)
    normed_all = gather_rows(layer_norm(hidden_wide, ln1_gain, ln1_shift).astype(jnp.bfloat16))
    projected = jnp.einsum("pnd,jdc->jpnc", normed_all, w_qkv, preferred_element_type=jnp.float32)
    queries = (projected[0] + b_qv[0]).astype(jnp.bfloat16)
    key_rows, value_rows = (
        lax.all_gather(projected[1].astype(jnp.bfloat16), "seq", axis=0, tiled=True),
        lax.all_gather((projected[2] + b_qv[1]).astype(jnp.bfloat16), "seq", axis=0, tiled=True),
    )
    attended, log_total = attend(queries, key_rows, value_rows, chosen_now, seq_start, seq_first)
    mixed_rows = (attended * query_mask[:, :, None]).astype(jnp.bfloat16)
    middle = hidden_wide + scatter_product(mixed_rows, w_out, "pnc,cd->pnd") + b_out
    normed_mlp = gather_rows(layer_norm(middle, ln2_gain, ln2_shift).astype(jnp.bfloat16))
    pre_active = (
        jnp.einsum("pnd,df->pnf", normed_mlp, w_fc, preferred_element_type=jnp.float32) + b_fc
    )
    active = gelu_tanh(pre_active).astype(jnp.bfloat16)
    if not finish:
        return (
            normed_all,
            queries,
            key_rows,
            value_rows,
            log_total,
            mixed_rows,
            middle,
            normed_mlp,
            pre_active,
            active,
        )
    output = (middle + scatter_product(active, w_proj, "pnf,fd->pnd") + b_proj).astype(jnp.bfloat16)
    return (output, (key_rows, value_rows))


def backward_pass(hidden, upstream, params, chosen_now, query_mask, seq_start, seq_first):
    (
        ln1_gain,
        ln1_shift,
        w_qkv,
        b_qv,
        w_out,
        b_out,
        ln2_gain,
        ln2_shift,
        w_fc,
        b_fc,
        w_proj,
        b_proj,
    ) = params
    (
        normed_all,
        queries,
        key_rows,
        value_rows,
        log_total,
        mixed_rows,
        middle,
        normed_mlp,
        pre_active,
        active,
    ) = forward_pass(hidden, params, chosen_now, query_mask, seq_start, seq_first, False)
    upstream_all = gather_rows(upstream)
    grad_w_proj = jnp.einsum(
        "pnf,pnd->fd", active, upstream_all, preferred_element_type=jnp.float32
    )
    grad_b_proj = jnp.sum(upstream.astype(jnp.float32), axis=(0, 1))
    grad_active = jnp.einsum(
        "pnd,fd->pnf", upstream_all, w_proj, preferred_element_type=jnp.float32
    )
    unused_value, gelu_pull = jax.vjp(gelu_tanh, pre_active)
    grad_pre = gelu_pull(grad_active)[0].astype(jnp.bfloat16)
    grad_w_fc = jnp.einsum("pnd,pnf->df", normed_mlp, grad_pre, preferred_element_type=jnp.float32)
    grad_b_fc = jnp.sum(grad_pre.astype(jnp.float32), axis=(0, 1))
    grad_normed_mlp = scatter_product(grad_pre, w_fc, "pnf,df->pnd")
    unused_norm, second_pull = jax.vjp(layer_norm, middle, ln2_gain, ln2_shift)
    grad_mid_norm, grad_ln2_gain, grad_ln2_shift = second_pull(grad_normed_mlp)
    grad_middle = upstream.astype(jnp.float32) + grad_mid_norm
    grad_branch = grad_middle.astype(jnp.bfloat16)
    grad_b_out = jnp.sum(grad_branch.astype(jnp.float32), axis=(0, 1))
    branch_all = gather_rows(grad_branch)
    grad_w_out = jnp.einsum(
        "pnc,pnd->cd", mixed_rows, branch_all, preferred_element_type=jnp.float32
    )
    grad_mixed = jnp.einsum(
        "pnd,cd->pnc", branch_all, w_out, preferred_element_type=jnp.float32
    ).astype(jnp.bfloat16) * query_mask[:, :, None].astype(jnp.bfloat16)
    grad_queries, key_grad_all, value_grad_all = attend_back(
        queries, key_rows, value_rows, chosen_now, seq_start, seq_first, log_total, grad_mixed
    )
    key_grad, value_grad = (
        lax.psum_scatter(
            key_grad_all.astype(jnp.bfloat16), "seq", scatter_dimension=0, tiled=True
        ).astype(jnp.float32),
        lax.psum_scatter(
            value_grad_all.astype(jnp.bfloat16), "seq", scatter_dimension=0, tiled=True
        ).astype(jnp.float32),
    )
    grad_project = jnp.stack(
        [
            grad_queries.astype(jnp.bfloat16),
            key_grad.astype(jnp.bfloat16),
            value_grad.astype(jnp.bfloat16),
        ],
        2,
    )
    grad_w_qkv = jnp.einsum(
        "pnd,pnjc->jdc", normed_all, grad_project, preferred_element_type=jnp.float32
    )
    grad_b_qv = jnp.sum(grad_project[:, :, 0::2].astype(jnp.float32), axis=(0, 1))
    grad_normed = scatter_product(grad_project, w_qkv, "pnjc,jdc->pnd")
    unused_first, first_pull = jax.vjp(layer_norm, hidden.astype(jnp.float32), ln1_gain, ln1_shift)
    grad_in_norm, grad_ln1_gain, grad_ln1_shift = first_pull(grad_normed)
    grad_hidden = (grad_middle + grad_in_norm).astype(jnp.bfloat16)
    block_grads = (
        grad_ln1_gain,
        grad_ln1_shift,
        grad_w_qkv,
        grad_b_qv,
        grad_w_out,
        grad_b_out,
        grad_ln2_gain,
        grad_ln2_shift,
        grad_w_fc,
        grad_b_fc,
        grad_w_proj,
        grad_b_proj,
    )
    return (grad_hidden, block_grads)


def on_device(
    inputs,
    cotangent,
    lengths,
    chosen,
    ln1_gain,
    ln1_shift,
    w_qkv,
    b_qv,
    w_out,
    b_out,
    ln2_gain,
    ln2_shift,
    w_fc,
    b_fc,
    w_proj,
    b_proj,
):
    params = tuple(
        (
            weight_array[0]
            for weight_array in (
                ln1_gain,
                ln1_shift,
                w_qkv,
                b_qv,
                w_out,
                b_out,
                ln2_gain,
                ln2_shift,
                w_fc,
                b_fc,
                w_proj,
                b_proj,
            )
        )
    )
    section_index = lax.axis_index("section")
    section_count = lax.axis_size("section")
    seq_index = lax.axis_index("seq")
    tensor_index = lax.axis_index("tensor")
    tensor_count = lax.axis_size("tensor")
    micro_count, rows_local, buckets, feature_width = inputs.shape
    length_local = rows_local * tensor_count
    heads_width = w_qkv.shape[-1]
    seq_start = seq_index * length_local
    seq_first = seq_index == 0
    positions = seq_start + lax.broadcasted_iota(jnp.int32, (micro_count, length_local, buckets), 1)
    mask_all = (positions < lengths[:, None, :]).astype(jnp.float32)
    mask_rows = lax.dynamic_slice_in_dim(mask_all, tensor_index * rows_local, rows_local, 1)
    step_count = micro_count + section_count - 1
    chosen_section = chosen[0]
    received = jnp.zeros((rows_local, buckets, feature_width), jnp.bfloat16)
    stored = jnp.zeros((micro_count, rows_local, buckets, feature_width), jnp.bfloat16)
    outputs = jnp.zeros_like(stored)
    for step_index in range(step_count):
        micro_index = step_index - section_index
        running = (micro_index >= 0) & (micro_index < micro_count)
        slot_index = jnp.clip(micro_index, 0, micro_count - 1)
        block_in = jnp.where(
            section_index == 0, lax.dynamic_index_in_dim(inputs, slot_index, 0, False), received
        )
        chosen_now = lax.dynamic_index_in_dim(chosen_section, slot_index, 0, False)
        query_mask = lax.dynamic_index_in_dim(mask_all, slot_index, 0, False)
        result, key_pair = forward_pass(
            block_in, params, chosen_now, query_mask, seq_start, seq_first, True
        )
        stored = jnp.where(
            running, lax.dynamic_update_index_in_dim(stored, block_in, slot_index, 0), stored
        )
        outputs = jnp.where(
            running, lax.dynamic_update_index_in_dim(outputs, result, slot_index, 0), outputs
        )
        received = from_behind(result, "section", 1)
    back_received = jnp.zeros((rows_local, buckets, feature_width), jnp.bfloat16)
    in_grads = jnp.zeros_like(stored)
    totals = None
    for step_index in range(step_count):
        micro_index = step_index - (section_count - 1 - section_index)
        running = (micro_index >= 0) & (micro_index < micro_count)
        slot_index = jnp.clip(micro_index, 0, micro_count - 1)
        chosen_now = lax.dynamic_index_in_dim(chosen_section, slot_index, 0, False)
        query_mask = lax.dynamic_index_in_dim(mask_all, slot_index, 0, False)
        local_mask = lax.dynamic_index_in_dim(mask_rows, slot_index, 0, False)
        top_grad = (
            lax.dynamic_index_in_dim(cotangent, slot_index, 0, False).astype(jnp.float32)
            * local_mask[:, :, None]
        ).astype(jnp.bfloat16)
        upstream = jnp.where(section_index == section_count - 1, top_grad, back_received)
        hidden = lax.dynamic_index_in_dim(stored, slot_index, 0, False)
        grad_hidden, block_grads = backward_pass(
            hidden, upstream, params, chosen_now, query_mask, seq_start, seq_first
        )
        block_grads = tuple(
            (jnp.where(running, grad_part, jnp.zeros_like(grad_part)) for grad_part in block_grads)
        )
        totals = (
            block_grads
            if step_index == 0
            else tuple(
                (total_part + grad_part for total_part, grad_part in zip(totals, block_grads))
            )
        )
        in_grads = jnp.where(
            running, lax.dynamic_update_index_in_dim(in_grads, grad_hidden, slot_index, 0), in_grads
        )
        back_received = from_behind(grad_hidden, "section", -1)
    (
        sum_ln1_gain,
        sum_ln1_shift,
        sum_w_qkv,
        sum_b_qv,
        sum_w_out,
        sum_b_out,
        sum_ln2_gain,
        sum_ln2_shift,
        sum_w_fc,
        sum_b_fc,
        sum_w_proj,
        sum_b_proj,
    ) = totals
    part_qkv, part_out, part_fc, part_proj = (
        lax.psum_scatter(
            sum_w_qkv.astype(jnp.bfloat16), "seq", scatter_dimension=1, tiled=True
        ).astype(jnp.float32),
        lax.psum_scatter(
            sum_w_out.astype(jnp.bfloat16), "seq", scatter_dimension=1, tiled=True
        ).astype(jnp.float32),
        lax.psum_scatter(
            sum_w_fc.astype(jnp.bfloat16), "seq", scatter_dimension=0, tiled=True
        ).astype(jnp.float32),
        lax.psum_scatter(
            sum_w_proj.astype(jnp.bfloat16), "seq", scatter_dimension=1, tiled=True
        ).astype(jnp.float32),
    )
    bias_qv = lax.dynamic_update_slice_in_dim(
        jnp.zeros((2, feature_width), jnp.float32), sum_b_qv, tensor_index * heads_width, 1
    )
    units_local = sum_b_fc.shape[0]
    bias_fc = lax.dynamic_update_slice_in_dim(
        jnp.zeros((units_local * tensor_count,), jnp.float32),
        sum_b_fc,
        tensor_index * units_local,
        0,
    )
    small_sums = lax.psum(
        (
            sum_ln1_gain,
            sum_ln1_shift,
            bias_qv,
            sum_b_out,
            sum_ln2_gain,
            sum_ln2_shift,
            bias_fc,
            sum_b_proj,
        ),
        ("seq", "tensor"),
    )
    return (
        outputs[None],
        in_grads[None],
        small_sums[0][None],
        small_sums[1][None],
        part_qkv[None],
        small_sums[2][None],
        part_out[None],
        small_sums[3][None],
        small_sums[4][None],
        small_sums[5][None],
        part_fc[None],
        small_sums[6][None],
        part_proj[None],
        small_sums[7][None],
    )


STREAMS = 4
NRM, NMLP, UPS, BRN, ACT, GPRE, MIX, DQKV = range(8)
F32 = jnp.float32
LOW = jnp.bfloat16
MESH_ID = pl.DeviceIdType.MESH


def dot_nn(left, right):
    return lax.dot_general(left, right, (((1,), (0,)), ((), ())), preferred_element_type=F32)


def dot_nt(left, right):
    return lax.dot_general(left, right, (((1,), (1,)), ((), ())), preferred_element_type=F32)


def dot_tn(left, right):
    return lax.dot_general(left, right, (((0,), (0,)), ((), ())), preferred_element_type=F32)


def standard(rows):
    centred = rows - jnp.mean(rows, axis=-1, keepdims=True)
    scale = lax.rsqrt(jnp.mean(centred * centred, axis=-1, keepdims=True) + NORM_EPS)
    return centred * scale, scale


def standard_back(grad, xhat, scale):
    inner = jnp.mean(grad * xhat, axis=-1, keepdims=True)
    return scale * (grad - jnp.mean(grad, axis=-1, keepdims=True) - xhat * inner)


def column_sum(rows):
    return jnp.sum(rows.astype(F32), axis=0, keepdims=True)


def relay_kernel(names, *refs):
    r = types.SimpleNamespace(**dict(zip(names, refs)))
    a, c, t = (lax.axis_index(name) for name in ("section", "seq", "tensor"))
    lines = lax.axis_size("section")
    chips = lax.axis_size("tensor")
    rows, buckets, width = r.inputs.shape[1:]
    half_width = width // 2
    local = rows * chips
    total = 2 * local
    stream_rows = local // STREAMS
    head_width = r.wo_in.shape[0]
    heads = head_width // HDIM
    blocks = local // QB
    units = r.wp_in.shape[0]
    scale = HDIM ** (-0.5)
    streams = range(STREAMS)

    def remote(src, dst, send, recv, **target):
        return pltpu.make_async_remote_copy(
            src_ref=src,
            dst_ref=dst,
            send_sem=send,
            recv_sem=recv,
            device_id=target,
            device_id_type=MESH_ID,
        )

    def drain(ref, sem):
        pltpu.make_async_copy(ref, ref, sem).wait()

    def row_block(index, size):
        return pl.ds(pl.multiple_of(index * size, size), size)

    near_chip = t + 1 - 2 * (t % 2)
    over_chip = (t + 2) % 4
    across_chip = 3 - t
    middle_chip = (t == 1) | (t == 2)
    end_chip = (t == 0) | (t == 3)
    owned = stream_rows // 2
    mine = row_block(t - 1, owned)
    my_half = row_block(c, local)

    barrier = pltpu.get_barrier_semaphore()
    for core in range(2):
        for step in range(1, chips):
            there = {"tensor": (t + step) % chips, "seq": core}
            pl.semaphore_signal(barrier, inc=1, device_id=there, device_id_type=MESH_ID)
        for step in range(1, lines):
            there = {"section": (a + step) % lines, "seq": core}
            pl.semaphore_signal(barrier, inc=1, device_id=there, device_id_type=MESH_ID)
    for step in range(1, lines):
        there = {"section": (a + step) % lines, "tensor": near_chip}
        pl.semaphore_signal(barrier, inc=1, device_id=there, device_id_type=MESH_ID)
    pl.semaphore_signal(barrier, inc=1, device_id={"seq": 1 - c}, device_id_type=MESH_ID)
    pl.semaphore_wait(barrier, 2 * (chips - 1) + 3 * (lines - 1) + 1)

    def beside(s):
        return s + 1 - 2 * (s % 2)

    def above(s):
        return (s + 2) % 4

    def store(p):
        return (r.wq, r.wo, r.wf, r.wp)[p]

    def source(p):
        return (r.wq_in, r.wo_in, r.wf_in, r.wp_in)[p]

    def height(p):
        return source(p).shape[0]

    def core_half(p, s, core):
        return store(p).at[s, row_block(core, height(p) // 2)]

    def first_hop(p, s, neighbour, which):
        return remote(
            source(p).at[row_block(c, height(p) // 2)],
            core_half(p, s, c),
            r.w_first_s.at[p, which],
            r.w_first_r.at[s, p],
            section=neighbour,
        )

    def second_hop(p, s, which):
        view = store(p).at[s, row_block(2 * c + which, height(p) // 4)]
        return remote(
            view, view, r.w_second_s.at[s, p], r.w_second_r.at[s, p, which], section=3 - s
        )

    def core_hop(p, s, core):
        view = core_half(p, s, core)
        return remote(view, view, r.w_core_s.at[s, p], r.w_core_r.at[s, p], seq=1 - c)

    def own_copy(p):
        return pltpu.make_async_copy(source(p), store(p).at[a], r.w_own.at[p])

    def pass_on(s, p, which):
        line = (beside(s), above(s))[which]

        @pl.when(a == line)
        def _():
            first_hop(p, s, line, which).wait_recv()
            second_hop(p, s, which).start()
            core_hop(p, s, c).start()

    def pass_later(pieces):
        for later in range(1, lines):
            for which in range(2):
                if (beside(later), above(later))[which] != 0:
                    for p in pieces:
                        pass_on(later, p, which)

    def pass_far(s, p):
        @pl.when(a == 3 - s)
        def _():
            second_hop(p, s, 0).wait_recv()
            second_hop(p, s, 1).wait_recv()
            core_hop(p, s, c).start()

    def need(s, p):
        @pl.when(s == 0)
        def _():
            pass_on(0, p, 0)
            pass_on(0, p, 1)
            pass_far(0, p)

        @pl.when(a == s)
        def _():
            own_copy(p).wait()

        @pl.when(a != s)
        def _():
            core_hop(p, s, 1 - c).wait_recv()

    def small_copy(step, line, slot):
        return remote(
            r.small_own, r.small.at[slot], r.small_s.at[step], r.small_r.at[slot], section=line
        )

    def count_copy(step, line, slot):
        return remote(
            r.count_own.at[line],
            r.count.at[slot],
            r.count_s.at[step],
            r.count_r.at[slot],
            section=line,
        )

    singles = (r.ln1_gain, r.ln1_shift, r.ln2_gain, r.ln2_shift, r.b_out, r.b_proj)
    for place, single in enumerate(singles):
        r.small_own[place : place + 1] = single[...]
    r.small_own[6:7, :units] = r.b_fc[...]
    r.small_own[7:8, :head_width] = r.b_qv[0:1]
    r.small_own[7:8, half_width : half_width + head_width] = r.b_qv[1:2]
    for step in range(1, lines):
        small_copy(step - 1, (a + step) % lines, a).start()
    for p in range(4):
        for which, line in enumerate((beside(a), above(a))):
            first_hop(p, a, line, which).start()
    for p in range(4):
        own_copy(p).start()
    r.small[a] = r.small_own[...]

    def place_of(index):
        inside = index % local
        stream, left = inside // stream_rows, inside % stream_rows
        first = (index // local) * local + (left // owned) * (local // 2)
        return first + stream * owned + left % owned

    def iota(shape, dimension):
        return lax.broadcasted_iota(jnp.int32, shape, dimension)

    square = jnp.where(iota((KSEL, KSEL), 0) == iota((KSEL, KSEL), 1), 1.0, 0.0).astype(LOW)
    position = place_of(iota((KSEL, total), 1)).astype(F32)
    for pair in range(lines * heads):
        line, head = pair // heads, pair % heads
        columns = dot_nt(square, r.chosen[pair].astype(F32).astype(LOW))
        for block in range(blocks):
            pick = head * blocks + block
            r.count_own[line, pick : pick + 1, :] = jnp.sum(
                jnp.where(columns[:, block : block + 1] == position, 1.0, 0.0),
                axis=0,
                keepdims=True,
            )
    for step in range(1, lines):
        count_copy(step - 1, (a + step) % lines, a).start()
    r.count[a] = r.count_own[a]

    NEAR, OVER, ACROSS = range(3)

    def gather(buffer, s, kind, j, owner, target, slot):
        view = buffer.at[s, j, row_block(owner - 1, owned)]
        return remote(
            view, view, r.ag_s.at[kind, j, slot], r.ag_r.at[kind, j, slot], tensor=target
        )

    def gather_start(buffer, s, kind, j):
        gather(buffer, s, kind, j, t, over_chip, OVER).start()
        gather(buffer, s, kind, j, t, across_chip, ACROSS).start()
        gather(buffer, s, kind, j, t, near_chip, NEAR).start()

    def gather_wait(buffer, s, kind, j):
        @pl.when(middle_chip)
        def _():
            gather(buffer, s, kind, j, across_chip, across_chip, ACROSS).wait_recv()

        @pl.when(end_chip)
        def _():
            gather(buffer, s, kind, j, near_chip, near_chip, NEAR).wait_recv()
            gather(buffer, s, kind, j, over_chip, over_chip, OVER).wait_recv()

    def gather_sent(buffer, s, kind, j):
        @pl.when(middle_chip)
        def _():
            gather(buffer, s, kind, j, t, over_chip, OVER).wait_send()
            gather(buffer, s, kind, j, t, across_chip, ACROSS).wait_send()
            gather(buffer, s, kind, j, t, near_chip, NEAR).wait_send()

    def scatter(s, kind, j, owner, slot):
        return remote(
            r.part.at[kind, j, row_block(owner - 1, owned)],
            r.arrived.at[s, kind, j, slot],
            r.rs_s.at[kind, j, slot],
            r.rs_r.at[kind, j, slot],
            tensor=owner,
        )

    def scatter_start(s, kind, j, product):
        r.part[kind, j] = product.astype(LOW)

        @pl.when(end_chip)
        def _():
            scatter(s, kind, j, over_chip, OVER).start()
            scatter(s, kind, j, near_chip, NEAR).start()

        @pl.when(middle_chip)
        def _():
            scatter(s, kind, j, across_chip, ACROSS).start()

    def scatter_sum(s, kind, j):
        result = r.part[kind, j, mine].astype(F32)
        for slot in (NEAR, ACROSS, OVER):
            scatter(s, kind, j, t, slot).wait_recv()
            result = result + r.arrived[s, kind, j, slot].astype(F32)
        return result

    def scatter_sent(s, kind, j):
        @pl.when(end_chip)
        def _():
            scatter(s, kind, j, over_chip, OVER).wait_send()
            scatter(s, kind, j, near_chip, NEAR).wait_send()

        @pl.when(middle_chip)
        def _():
            scatter(s, kind, j, across_chip, ACROSS).wait_send()

    own_rows = (r.nrm, r.nmlp, r.ups, r.brn, r.act, r.gpre, r.mix, r.dqkv)
    all_rows = (
        r.all_nrm,
        r.all_nmlp,
        r.all_ups,
        r.all_brn,
        r.all_act,
        r.all_gpre,
        r.all_mix,
        r.all_dqkv,
    )

    def rows_copy(index, s, same, stays=False):
        core = c if same else 1 - c
        src = own_rows[index].at[s]
        dst = all_rows[index].at[a, c]
        if index <= BRN:
            src = src.at[:, :, row_block(core, half_width)]
        recv = r.rows_r.at[index]
        if stays:
            return pltpu.make_async_copy(src, dst, recv)
        if same:
            return remote(src, dst, r.rows_s.at[index, s, 0], recv, section=s)
        return remote(src, dst, r.rows_s.at[index, s, 1], recv, section=s, seq=1 - c)

    passed_rows = {UPS: r.pass_ups, GPRE: r.pass_gpre, BRN: r.pass_brn, DQKV: r.pass_dqkv}
    passer = (a == 1) & (c == 1)

    def detours(index, s):
        return (a == 3) & (c == 1) & (s == 0) if index in passed_rows else False

    def detour_copy(index):
        place = tuple(passed_rows).index(index)
        return remote(
            own_rows[index].at[0],
            passed_rows[index],
            r.pass_s.at[place],
            r.pass_r.at[place],
            section=1,
        )

    def pass_rows(index):
        @pl.when(passer)
        def _():
            detour_copy(index).wait_recv()
            passed_copies(index, lambda copy: copy.start())

    def passed_copies(index, act):
        place = tuple(passed_rows).index(index)
        for step in range(2 if index <= BRN else 1):
            core = (c + step) % 2
            src = passed_rows[index]
            if index <= BRN:
                src = src.at[:, :, row_block(core, half_width)]
            act(
                remote(
                    src,
                    all_rows[index].at[3, c],
                    r.pass_on_s.at[place, step],
                    r.rows_r.at[index],
                    section=0,
                    seq=core,
                )
            )

    def rows_start(index, s):
        @pl.when(a == s)
        def _():
            rows_copy(index, s, True, True).start()

        if index in passed_rows:

            @pl.when(detours(index, s))
            def _():
                detour_copy(index).start()

            sends = jnp.logical_not(detours(index, s))
        else:
            sends = True

        @pl.when((a != s) & sends)
        def _():
            rows_copy(index, s, True).start()

        if index <= BRN:

            @pl.when(sends)
            def _():
                rows_copy(index, s, False).start()

    def forward_rows(s):
        for index in (NRM, MIX, NMLP, ACT):
            rows_start(index, s)

    def rows_sent(index, s):
        if index in passed_rows:

            @pl.when(detours(index, s))
            def _():
                detour_copy(index).wait_send()

            @pl.when(passer & (s == 0))
            def _():
                passed_copies(index, lambda copy: copy.wait_send())

            sends = jnp.logical_not(detours(index, s))
        else:
            sends = True

        @pl.when((a != s) & sends)
        def _():
            rows_copy(index, s, True).wait_send()

        if index <= BRN:

            @pl.when(sends)
            def _():
                rows_copy(index, s, False).wait_send()

    def share_copy(index, core):
        view = all_rows[index].at[:, core]
        return remote(view, view, r.share_s.at[index - ACT], r.share_r.at[index - ACT], seq=1 - c)

    def share(index):
        drain(all_rows[index].at[:, c], r.rows_r.at[index])
        share_copy(index, c).start()

    def norm_copy(s):
        return remote(
            r.norm_part.at[s], r.norm_all.at[a], r.norm_s.at[s], r.norm_r, section=s
        )

    def norm_start(s):
        @pl.when(a == s)
        def _():
            pltpu.make_async_copy(r.norm_part.at[s], r.norm_all.at[a], r.norm_r).start()

        @pl.when(a != s)
        def _():
            norm_copy(s).start()

    def home_copy(what, s, chip):
        src, dst, send, recv = what
        return remote(
            src.at[s, chip % 2],
            dst.at[a],
            send.at[s, chip % 2],
            recv,
            section=s,
            tensor=chip,
        )

    def home_start(what, s):
        src, dst, send, recv = what

        @pl.when(middle_chip & (a == s))
        def _():
            pltpu.make_async_copy(src.at[s, t % 2], dst.at[a], recv).start()

        @pl.when(middle_chip & (a != s))
        def _():
            home_copy(what, s, t).start()

        @pl.when(middle_chip)
        def _():
            home_copy(what, s, near_chip).start()

    def home_sent(what, s):
        @pl.when(middle_chip & (a != s))
        def _():
            home_copy(what, s, t).wait_send()

        @pl.when(middle_chip)
        def _():
            home_copy(what, s, near_chip).wait_send()

    out_home = (r.out_low, r.acts, r.out_s, r.out_r)
    grad_home = (r.grad_low, r.grads, r.grad_s, r.grad_r)

    length = r.lengths[a // buckets, a % buckets]
    key = place_of(iota((stream_rows, total), 1))
    for j in streams:
        query = place_of(c * local + j * stream_rows + iota((stream_rows, total), 0))
        r.near[j] = jnp.where((query >= key) & (query - key < WIN), 1.0, 0.0)
    key_row = place_of(iota((1, total), 1))

    def row_mask(place):
        return jnp.where(place < length, 1.0, 0.0)

    def multiplicity(s, j, head):
        far = []
        for block in range(blocks):
            pick = head * blocks + block
            limit = (c * blocks + block) * QB - WIN
            counted = jnp.where(key_row <= limit, r.count[s, pick : pick + 1, :], 0.0)
            far.append(jnp.broadcast_to(counted, (stream_rows // blocks, total)))
        return r.near[j] + jnp.concatenate(far, axis=0)

    def head_cols(head):
        return slice(head * HDIM, (head + 1) * HDIM)

    def kv_copy(s):
        view = r.kv.at[s, :, 0:local]
        return remote(view, view, r.kv_s.at[s], r.kv_r.at[s], seq=1 - c)

    def dkv_copy(s):
        return remote(r.dkv_out.at[s], r.dkv_in.at[s], r.dkv_s.at[s], r.dkv_r.at[s], seq=1 - c)

    def own_sequence(ref):
        both = ref[a // buckets].astype(F32)
        picked = both[:, 0, :]
        for bucket in range(1, buckets):
            picked = jnp.where(a % buckets == bucket, both[:, bucket, :], picked)
        return picked

    def own_part(j):
        chip, first = (j * owned) // rows, (j * owned) % rows
        return chip, slice(first, first + owned)

    def first_copy():
        return remote(r.first_out, r.first_in, r.first_s, r.first_r, tensor=near_chip)

    own_place = c * local + t * rows + iota((rows, 1), 0)
    r.first_out[0] = own_sequence(r.inputs).astype(LOW)
    r.first_out[1] = (own_sequence(r.cotangent) * row_mask(own_place)).astype(LOW)
    r.norm_part[...] = jnp.zeros_like(r.norm_part)

    @pl.when(c == 0)
    def _():
        r.kv[:, :, local:total] = jnp.zeros((lines, 2, local, head_width), LOW)


    @pl.when(end_chip)
    def _():
        first_copy().start()

    @pl.when(middle_chip)
    def _():
        first_copy().wait_recv()
        for which in range(2):
            here, beside_it = r.first_out[which].astype(F32), r.first_in[which].astype(F32)
            lower = jnp.where(t % 2 == 0, here, beside_it)
            upper = jnp.where(t % 2 == 0, beside_it, here)
            for j in streams:
                chip, part = own_part(j)
                own_block = (lower, upper)[chip][part]
                if which == 0:
                    r.hidden[j] = own_block
                else:
                    r.upstream[j] = own_block.astype(LOW)

    def on_owner(stage):
        def run(s, j):
            @pl.when(middle_chip)
            def _():
                stage(s, j)

        return run

    def keep_rows(target, s, j, result):
        chip, part = own_part(j)
        target[s, chip, part] = result

    @on_owner
    def enter(s, j):
        xhat, inverse = standard(r.hidden[j])
        r.xhat1[s, j] = xhat
        r.inv1[s, j] = jnp.broadcast_to(inverse, (owned, 128))
        r.nrm[s, j, mine] = (xhat * r.small[s, 0:1] + r.small[s, 1:2]).astype(LOW)
        gather_start(r.nrm, s, 0, j)

    def project(s, j):
        gather_wait(r.nrm, s, 0, j)
        normed = r.nrm[s, j]
        place = row_block(c * STREAMS + j, stream_rows)
        bias_v = r.small[s, 7:8, half_width : half_width + head_width]
        key_rows = dot_nt(normed, r.wq[s, head_width : 2 * head_width])
        value_rows = dot_nt(normed, r.wq[s, 2 * head_width : 3 * head_width]) + bias_v
        r.kv[s, 0, place] = key_rows.astype(LOW)
        r.kv[s, 1, place] = value_rows.astype(LOW)
        gather_sent(r.nrm, s, 0, j)

    def ask(s, j):
        queries = dot_nt(r.nrm[s, j], r.wq[s, 0:head_width]) + r.small[s, 7:8, :head_width]
        r.qry[s, j] = queries.astype(LOW)

    def attend_line(s, j):
        mixed = []
        for head in range(heads):
            cols = head_cols(head)
            times = multiplicity(s, j, head)
            scores = scale * dot_nt(r.qry[s, j, :, cols], r.kv[s, 0, :, cols])
            scores = jnp.where(times > 0.0, scores, MASKED)
            top = jnp.max(scores, axis=-1, keepdims=True)
            terms = times * jnp.exp(scores - top)
            weights = terms / jnp.sum(terms, axis=-1, keepdims=True)
            r.soft[s, j, head] = weights
            mixed.append(dot_nn(weights.astype(LOW), r.kv[s, 1, :, cols]))
        mask = row_mask(place_of(c * local + j * stream_rows + iota((stream_rows, 1), 0)))
        r.mix[s, j] = (jnp.concatenate(mixed, axis=-1) * mask).astype(LOW)

    def leave_attention(s, j):
        scatter_start(s, 0, j, dot_nn(r.mix[s, j], r.wo[s]))

    @on_owner
    def between(s, j):
        middle = r.hidden[j] + scatter_sum(s, 0, j) + r.small[s, 4:5]
        r.middle[j] = middle
        xhat, inverse = standard(middle)
        r.xhat2[s, j] = xhat
        r.inv2[s, j] = jnp.broadcast_to(inverse, (owned, 128))
        r.nmlp[s, j, mine] = (xhat * r.small[s, 2:3] + r.small[s, 3:4]).astype(LOW)
        gather_start(r.nmlp, s, 1, j)

    def feed(s, j):
        gather_wait(r.nmlp, s, 1, j)
        before = dot_nn(r.nmlp[s, j], r.wf[s]) + r.small[s, 6:7, :units]
        bend = jnp.tanh(0.7978845608028654 * (before + 0.044715 * before * before * before))
        r.act[s, j] = (0.5 * before * (1.0 + bend)).astype(LOW)
        r.slope[s, j] = 0.5 * (1.0 + bend) + 0.5 * before * (1.0 - bend * bend) * (
            0.7978845608028654 * (1.0 + 3 * 0.044715 * before * before)
        )

        gather_sent(r.nmlp, s, 1, j)

    def leave_feed(s, j):
        scatter_start(s, 1, j, dot_nn(r.act[s, j], r.wp[s]))

    @on_owner
    def finish(s, j):
        result = r.middle[j] + scatter_sum(s, 1, j) + r.small[s, 5:6]
        keep_rows(r.out_low, s, j, result.astype(LOW))
        r.hidden[j] = result.astype(LOW).astype(F32)

    def small_ready(s):
        @pl.when(a != s)
        def _():
            small_copy(0, a, s).wait_recv()

    small_ready(0)
    for j in streams:
        enter(0, j)

    def forward(s, _):
        need(s, 0)
        for j in streams:
            project(s, j)

        @pl.when(c == 0)
        def _():
            kv_copy(s).start()

        for j in streams:
            ask(s, j)

        @pl.when(a != s)
        def _():
            count_copy(0, a, s).wait_recv()

        @pl.when(c == 1)
        def _():
            kv_copy(s).wait_recv()

        for j in streams:
            attend_line(s, j)
            if j == 0:
                need(s, 1)
            leave_attention(s, j)

        @pl.when(s == 0)
        def _():
            pass_later((0, 1))

        @pl.when(s == 1)
        def _():
            pass_on(1, 2, 0)
            pass_on(1, 3, 0)
            for p in range(4):
                pass_on(2, p, 1)

        @pl.when(s > 0)
        def _():
            pass_far(s, 2)
            pass_far(s, 3)

        for j in streams:
            between(s, j)
            scatter_sent(s, 0, j)
        need(s, 2)

        @pl.when(s == 0)
        def _():
            pass_later((2,))

        for j in streams:
            feed(s, j)
            if j == 0:
                need(s, 3)
            leave_feed(s, j)

        @pl.when(s == 0)
        def _():
            pass_later((3,))


        @pl.when(s >= 2)
        def _():
            forward_rows(s - 2)


        @pl.when(s + 1 < lines)
        def _():
            small_ready(s + 1)

        for j in streams:
            finish(s, j)
            scatter_sent(s, 1, j)

            @pl.when(s + 1 < lines)
            def _():
                enter(s + 1, j)

        home_start(out_home, s)

        @pl.when(s == 0)
        def _():
            pass_on(1, 0, 0)
            pass_on(1, 1, 0)

        @pl.when(s + 1 < lines)
        def _():
            pass_far(s + 1, 0)
            pass_far(s + 1, 1)

        return 0

    lax.fori_loop(0, lines, forward, 0)

    @on_owner
    def turn(s, j):
        upstream = r.upstream[j]
        r.ups[s, j, mine] = upstream
        gather_start(r.ups, s, 2, j)
        r.norm_part[s, 5:6] += column_sum(upstream)

    def feed_back(s, j):
        gather_wait(r.ups, s, 2, j)
        grad_pre = (dot_nt(r.ups[s, j], r.wp[s]) * r.slope[s, j]).astype(LOW)
        r.gpre[s, j] = grad_pre
        scatter_start(s, 2, j, dot_nt(grad_pre, r.wf[s]))
        r.norm_part[s, 6:7, :units] += column_sum(grad_pre)
        gather_sent(r.ups, s, 2, j)

    @on_owner
    def between_back(s, j):
        grad = scatter_sum(s, 2, j)
        xhat = r.xhat2[s, j]
        upstream = r.upstream[j].astype(F32)
        grad_middle = upstream + standard_back(
            grad * r.small[s, 2:3], xhat, r.inv2[s, j, :, 0:1]
        )
        r.middle[j] = grad_middle
        branch = grad_middle.astype(LOW)
        r.brn[s, j, mine] = branch
        gather_start(r.brn, s, 3, j)
        r.norm_part[s, 2:3] += column_sum(grad * xhat)
        r.norm_part[s, 3:4] += column_sum(grad)
        r.norm_part[s, 4:5] += column_sum(branch)

    def mixed_back(s, j):
        gather_wait(r.brn, s, 3, j)
        place = place_of(c * local + j * stream_rows + iota((stream_rows, 1), 0))
        r.gmix[j] = (dot_nt(r.brn[s, j], r.wo[s]) * row_mask(place)).astype(LOW)
        gather_sent(r.brn, s, 3, j)

    def attend_line_back(s, j):
        grad_q, grad_k, grad_v = [], [], []
        for head in range(heads):
            cols = head_cols(head)
            weights = r.soft[s, j, head]
            grad_head = r.gmix[j, :, cols]
            grad_weights = dot_nt(grad_head, r.kv[s, 1, :, cols])
            inner = jnp.sum(weights * grad_weights, axis=-1, keepdims=True)
            grad_scores = (weights * (grad_weights - inner)).astype(LOW)
            grad_k.append(scale * dot_tn(grad_scores, r.qry[s, j, :, cols]))
            grad_v.append(dot_tn(weights.astype(LOW), grad_head))
            grad_q.append(scale * dot_nn(grad_scores, r.kv[s, 0, :, cols]))
        for which, grad in enumerate((grad_k, grad_v)):
            grad = jnp.concatenate(grad, axis=-1)
            r.dkv_all[which] = grad if j == 0 else r.dkv_all[which] + grad
        grad_q = jnp.concatenate(grad_q, axis=-1).astype(LOW)
        r.dqkv[s, 0, j] = grad_q
        r.norm_part[s, 7:8, :head_width] += column_sum(grad_q)

    def join_keys(s):
        @pl.when(c == 1)
        def _():
            r.dkv_out[s] = r.dkv_all[:, 0:local].astype(LOW)
            dkv_copy(s).start()

        @pl.when(c == 0)
        def _():
            dkv_copy(s).wait_recv()
            r.dkv_all[:, 0:local] += r.dkv_in[s].astype(F32)

        for which in range(2):
            joined = r.dkv_all[which, my_half].astype(LOW)
            r.dqkv[s, 1 + which] = joined.reshape(r.dqkv.shape[2:])
            if which == 1:
                r.norm_part[s, 7:8, half_width : half_width + head_width] = column_sum(joined)

    def leave_back(s, j):
        product = dot_nn(r.dqkv[s, 0, j], r.wq[s, 0:head_width])
        for which in range(1, 3):
            weight = r.wq[s, which * head_width : (which + 1) * head_width]
            product = product + dot_nn(r.dqkv[s, which, j], weight)
        scatter_start(s, 3, j, product)

    @on_owner
    def finish_back(s, j):
        grad = scatter_sum(s, 3, j)
        xhat = r.xhat1[s, j]
        result = r.middle[j] + standard_back(
            grad * r.small[s, 0:1], xhat, r.inv1[s, j, :, 0:1]
        )
        r.upstream[j] = result.astype(LOW)
        keep_rows(r.grad_low, s, j, result.astype(LOW))
        r.norm_part[s, 0:1] += column_sum(grad * xhat)
        r.norm_part[s, 1:2] += column_sum(grad)

    for j in streams:
        turn(lines - 1, j)

    def backward(index, _):
        s = lines - 1 - index
        for j in streams:
            feed_back(s, j)
        rows_start(UPS, s)
        rows_start(GPRE, s)

        @pl.when(index < 2)
        def _():
            forward_rows(lines - 2 + index)

        @pl.when(index == lines - 1)
        def _():
            share(ACT)
            share(MIX)

        for j in streams:
            between_back(s, j)
            scatter_sent(s, 2, j)
        for j in streams:
            mixed_back(s, j)
            attend_line_back(s, j)
        join_keys(s)
        rows_start(BRN, s)

        @pl.when(s == 0)
        def _():
            pass_rows(UPS)
            pass_rows(GPRE)

        for j in streams:
            leave_back(s, j)
        rows_start(DQKV, s)
        for j in streams:
            finish_back(s, j)
            scatter_sent(s, 3, j)

            @pl.when(s > 0)
            def _():
                turn(s - 1, j)

        norm_start(s)
        home_start(grad_home, s)
        return 0

    lax.fori_loop(0, lines, backward, 0)

    pass_rows(BRN)
    pass_rows(DQKV)
    share(GPRE)
    share(DQKV)

    drain(r.norm_all, r.norm_r)
    slot = c * chips + t
    norm_sum = r.norm_all[0]
    for line in range(1, lines):
        norm_sum = norm_sum + r.norm_all[line]
    r.ends[slot] = norm_sum

    def ends_copy(step):
        core, chip = step // chips, step % chips
        view = r.ends.at[slot]
        return remote(
            view,
            view,
            r.ends_s.at[step - 1],
            r.ends_r,
            seq=(c + core) % 2,
            tensor=(t + chip) % chips,
        )

    for step in range(1, 2 * chips):
        ends_copy(step).start()

    for index in range(ACT):
        drain(all_rows[index], r.rows_r.at[index])
    for index in range(ACT, 8):
        share_copy(index, 1 - c).wait_recv()
        share_copy(index, c).wait_send()
    drain(r.acts, r.out_r)
    drain(r.grads, r.grad_r)
    drain(r.ends.at[0 : 2 * chips - 1], r.ends_r)
    for step in range(1, 2 * chips):
        ends_copy(step).wait_send()
    for step in range(1, lines):
        small_copy(step - 1, (a + step) % lines, a).wait_send()
        count_copy(step - 1, (a + step) % lines, a).wait_send()
    for p in range(4):
        for which, line in enumerate((beside(a), above(a))):
            first_hop(p, a, line, which).wait_send()

    @pl.when(end_chip)
    def _():
        first_copy().wait_send()

    def sent(s, _):
        home_sent(out_home, s)
        home_sent(grad_home, s)

        @pl.when(a != s)
        def _():
            norm_copy(s).wait_send()

        @pl.when(c == 0)
        def _():
            kv_copy(s).wait_send()

        @pl.when(c == 1)
        def _():
            dkv_copy(s).wait_send()

        for index in range(8):
            rows_sent(index, s)
        for p in range(4):

            @pl.when((a == beside(s)) | (a == above(s)))
            def _():
                second_hop(p, s, 0).wait_send()

            @pl.when(a != s)
            def _():
                core_hop(p, s, c).wait_send()

        return 0

    lax.fori_loop(0, lines, sent, 0)


def relay_call(inputs, cotangent, lengths, chosen, singles, weights):
    lines = lax.axis_size("section")
    chips = lax.axis_size("tensor")
    rows, buckets, width = inputs.shape[1:]
    local, total, half = rows * chips, 2 * rows * chips, width // 2
    head_width, units = weights["wo_in"].shape[0], weights["wp_in"].shape[0]
    heads = head_width // HDIM
    stream = local // STREAMS
    peers, owned = chips - 1, stream // 2
    vmem, dma = pltpu.VMEM, pltpu.SemaphoreType.DMA
    operands = dict(
        inputs=inputs,
        cotangent=cotangent,
        lengths=lengths,
        chosen=chosen,
        **singles,
        **weights,
    )

    def space(name):
        if name in weights:
            return pl.ANY
        return pltpu.SMEM if operands[name] is lengths else pltpu.VMEM

    sums = dict(
        acts=((lines, rows, width), LOW),
        grads=((lines, rows, width), LOW),
        ends=((2 * chips, 8, width), F32),
    )
    gathered = dict(
        all_nrm=((lines, 2, STREAMS, stream, half), LOW),
        all_nmlp=((lines, 2, STREAMS, stream, half), LOW),
        all_ups=((lines, 2, STREAMS, stream, half), LOW),
        all_brn=((lines, 2, STREAMS, stream, half), LOW),
        all_act=((lines, 2, STREAMS, stream, units), LOW),
        all_gpre=((lines, 2, STREAMS, stream, units), LOW),
        all_mix=((lines, 2, STREAMS, stream, head_width), LOW),
        all_dqkv=((lines, 2, 3, STREAMS, stream, head_width), LOW),
    )
    outputs = dict(**sums, **gathered)
    scratch = dict(
        wq=vmem((lines,) + weights["wq_in"].shape, LOW),
        wo=vmem((lines,) + weights["wo_in"].shape, LOW),
        wf=vmem((lines,) + weights["wf_in"].shape, LOW),
        wp=vmem((lines,) + weights["wp_in"].shape, LOW),
        small_own=vmem((8, width), F32),
        small=vmem((lines, 8, width), F32),
        count_own=vmem((lines, 8, total), F32),
        count=vmem((lines, 8, total), F32),
        hidden=vmem((STREAMS, owned, width), F32),
        middle=vmem((STREAMS, owned, width), F32),
        upstream=vmem((STREAMS, owned, width), LOW),
        first_out=vmem((2, rows, width), LOW),
        first_in=vmem((2, rows, width), LOW),
        xhat1=vmem((lines, STREAMS, owned, width), F32),
        inv1=vmem((lines, STREAMS, owned, 128), F32),
        xhat2=vmem((lines, STREAMS, owned, width), F32),
        inv2=vmem((lines, STREAMS, owned, 128), F32),
        nrm=vmem((lines, STREAMS, stream, width), LOW),
        nmlp=vmem((lines, STREAMS, stream, width), LOW),
        ups=vmem((lines, STREAMS, stream, width), LOW),
        brn=vmem((lines, STREAMS, stream, width), LOW),
        act=vmem((lines, STREAMS, stream, units), LOW),
        gpre=vmem((lines, STREAMS, stream, units), LOW),
        slope=vmem((lines, STREAMS, stream, units), F32),
        mix=vmem((lines, STREAMS, stream, head_width), LOW),
        qry=vmem((lines, STREAMS, stream, head_width), LOW),
        gmix=vmem((STREAMS, stream, head_width), LOW),
        dqkv=vmem((lines, 3, STREAMS, stream, head_width), LOW),
        pass_ups=vmem((STREAMS, stream, width), LOW),
        pass_gpre=vmem((STREAMS, stream, units), LOW),
        pass_brn=vmem((STREAMS, stream, width), LOW),
        pass_dqkv=vmem((3, STREAMS, stream, head_width), LOW),
        kv=vmem((lines, 2, total, head_width), LOW),
        soft=vmem((lines, STREAMS, heads, stream, total), F32),
        near=vmem((STREAMS, stream, total), F32),
        dkv_all=vmem((2, total, head_width), F32),
        dkv_out=vmem((lines, 2, local, head_width), LOW),
        dkv_in=vmem((lines, 2, local, head_width), LOW),
        part=vmem((4, STREAMS, stream, width), LOW),
        arrived=vmem((lines, 4, STREAMS, peers, owned, width), LOW),
        out_low=vmem((lines, 2, rows, width), LOW),
        grad_low=vmem((lines, 2, rows, width), LOW),
        norm_part=vmem((lines, 8, width), F32),
        norm_all=vmem((lines, 8, width), F32),
        w_first_s=dma((4, 2)),
        w_first_r=dma((lines, 4)),
        w_second_s=dma((lines, 4)),
        w_second_r=dma((lines, 4, 2)),
        w_core_s=dma((lines, 4)),
        w_core_r=dma((lines, 4)),
        w_own=dma((4,)),
        small_s=dma((lines - 1,)),
        small_r=dma((lines,)),
        count_s=dma((lines - 1,)),
        count_r=dma((lines,)),
        ag_s=dma((4, STREAMS, peers)),
        ag_r=dma((4, STREAMS, peers)),
        rs_s=dma((4, STREAMS, peers)),
        rs_r=dma((4, STREAMS, peers)),
        kv_s=dma((lines,)),
        kv_r=dma((lines,)),
        dkv_s=dma((lines,)),
        dkv_r=dma((lines,)),
        rows_s=dma((8, lines, 2)),
        rows_r=dma((8,)),
        pass_s=dma((4,)),
        pass_r=dma((4,)),
        pass_on_s=dma((4, 2)),
        share_s=dma((4,)),
        share_r=dma((4,)),
        first_s=dma,
        first_r=dma,
        out_s=dma((lines, 2)),
        out_r=dma,
        grad_s=dma((lines, 2)),
        grad_r=dma,
        norm_s=dma((lines,)),
        norm_r=dma,
        ends_s=dma((2 * chips - 1,)),
        ends_r=dma,
    )
    names = tuple(operands) + tuple(outputs) + tuple(scratch)
    results = pl.pallas_call(
        functools.partial(relay_kernel, names),
        out_shape=[jax.ShapeDtypeStruct(shape, kind) for shape, kind in outputs.values()],
        in_specs=[pl.BlockSpec(memory_space=space(name)) for name in operands],
        out_specs=[
            pl.BlockSpec(memory_space=pl.ANY if name in gathered else pltpu.VMEM)
            for name in outputs
        ],
        scratch_shapes=list(scratch.values()),
        compiler_params=pltpu.CompilerParams(
            collective_id=0, has_side_effects=True, vmem_limit_bytes=60 * 2**20
        ),
        name="relay",
    )(*operands.values())
    return dict(zip(outputs, results))


def weights_kernel(names, *refs):
    r = types.SimpleNamespace(**dict(zip(names, refs)))
    step = pl.program_id(0)
    micro_count, rows, buckets, width = r.activations.shape
    chips, units, head_width = r.ends.shape[0] // 2, r.all_act.shape[-1], r.all_mix.shape[-1]

    @pl.when(step == 0)
    def _():
        sums = r.ends[0]
        for other in range(1, 2 * chips):
            sums = sums + r.ends[other]
        singles = (r.ln1_gain, r.ln1_shift, r.ln2_gain, r.ln2_shift, r.b_out, r.b_proj)
        for place, single in enumerate(singles):
            single[...] = sums[place : place + 1]
        for chip in range(chips):
            both = r.ends[chip] + r.ends[chips + chip]
            r.b_fc[:, chip * units : (chip + 1) * units] = both[6:7, :units]
            here = slice(chip * head_width, (chip + 1) * head_width)
            r.b_qv[0:1, here] = both[7:8, :head_width]
            r.b_qv[1:2, here] = both[7:8, width // 2 : width // 2 + head_width]
        for target, source in ((r.activations, r.acts), (r.in_grads, r.grads)):
            for micro in range(micro_count):
                rows_of = [
                    source[micro * buckets + bucket].astype(F32)[:, None, :]
                    for bucket in range(buckets)
                ]
                target[micro] = jnp.concatenate(rows_of, axis=1).astype(LOW)
        for target in (r.w_qkv, r.w_out, r.w_fc, r.w_proj):
            target[...] = jnp.zeros_like(target)

    def rows_of_sequence(ref):
        return ref[0].reshape(2 * chips * rows, ref.shape[-1])

    nrm, nmlp, ups, brn, act, gpre, mix = (
        rows_of_sequence(ref)
        for ref in (r.all_nrm, r.all_nmlp, r.all_ups, r.all_brn, r.all_act, r.all_gpre, r.all_mix)
    )
    r.w_proj[...] += dot_tn(act, ups)
    r.w_fc[...] += dot_tn(nmlp, gpre)
    r.w_out[...] += dot_tn(mix, brn)
    for which in range(3):
        grad = r.all_dqkv[0, :, which].reshape(2 * chips * rows, head_width)
        r.w_qkv[which] += dot_tn(grad, nrm)


def weights_call(relayed, inputs_shape, head_width, units):
    lines = lax.axis_size("section")
    chips = lax.axis_size("tensor")
    width = inputs_shape[-1]
    half = width // 2
    outputs = dict(
        activations=(inputs_shape, LOW),
        in_grads=(inputs_shape, LOW),
        ln1_gain=((1, width), F32),
        ln1_shift=((1, width), F32),
        w_qkv=((3, head_width, half), F32),
        b_qv=((2, width), F32),
        w_out=((head_width, half), F32),
        b_out=((1, width), F32),
        ln2_gain=((1, width), F32),
        ln2_shift=((1, width), F32),
        w_fc=((half, units), F32),
        b_fc=((1, chips * units), F32),
        w_proj=((units, half), F32),
        b_proj=((1, width), F32),
    )

    def spec(array):
        if len(array.shape) < 5:
            return pl.BlockSpec(array.shape, lambda step: (0,) * len(array.shape))
        return pl.BlockSpec(
            (1,) + array.shape[1:], lambda step: (step,) + (0,) * (len(array.shape) - 1)
        )

    def whole(shape):
        return pl.BlockSpec(shape, lambda step: (0,) * len(shape))

    return pl.pallas_call(
        functools.partial(weights_kernel, tuple(relayed) + tuple(outputs)),
        out_shape=[jax.ShapeDtypeStruct(shape, kind) for shape, kind in outputs.values()],
        grid=(lines,),
        in_specs=[spec(array) for array in relayed.values()],
        out_specs=[whole(shape) for shape, _ in outputs.values()],
        compiler_params=pltpu.CompilerParams(vmem_limit_bytes=60 * 2**20),
        name="weight_gradients",
    )(*relayed.values())


def on_line(
    inputs,
    cotangent,
    lengths,
    chosen,
    ln1_gain,
    ln1_shift,
    w_qkv,
    b_qv,
    w_out,
    b_out,
    ln2_gain,
    ln2_shift,
    w_fc,
    b_fc,
    w_proj,
    b_proj,
):
    head_width, units = w_out.shape[1], w_fc.shape[2]
    singles = dict(
        ln1_gain=ln1_gain,
        ln1_shift=ln1_shift,
        ln2_gain=ln2_gain,
        ln2_shift=ln2_shift,
        b_out=b_out,
        b_proj=b_proj,
        b_fc=b_fc,
        b_qv=b_qv[0],
    )
    weights = dict(
        wq_in=jnp.swapaxes(w_qkv[0], 1, 2).reshape(-1, inputs.shape[-1]),
        wo_in=w_out[0],
        wf_in=w_fc[0],
        wp_in=w_proj[0],
    )
    picks = chosen.reshape((-1,) + chosen.shape[-2:])
    relayed = relay_call(inputs, cotangent, lengths, picks, singles, weights)
    results = list(weights_call(relayed, inputs.shape, head_width, units))
    results[4] = jnp.swapaxes(results[4], 1, 2)
    vectors = (2, 3, 7, 8, 9, 11, 13)
    return tuple(
        result if place in vectors else result[None] for place, result in enumerate(results)
    )


def fits_lines(mesh):
    return mesh.shape["section"] == 4 and mesh.shape["seq"] == 2 and mesh.shape["tensor"] == 4


def solution(mesh):
    placed = (
        P(None, ("seq", "tensor"), None, None),
        P(None, ("seq", "tensor"), None, None),
        P(),
        P("section", None, None, "tensor", "seq", None),
        P("section", None),
        P("section", None),
        P("section", None, None, "tensor"),
        P("section", None, "tensor"),
        P("section", "tensor", None),
        P("section", None),
        P("section", None),
        P("section", None),
        P("section", None, "tensor"),
        P("section", "tensor"),
        P("section", "tensor", None),
        P("section", None),
    )
    return jax.shard_map(
        on_line if fits_lines(mesh) else on_device,
        mesh=mesh,
        in_specs=placed,
        out_specs=(
            P("section", None, ("seq", "tensor"), None, None),
            P("section", None, ("seq", "tensor"), None, None),
            P("section", None),
            P("section", None),
            P("section", None, "seq", "tensor"),
            P("section", None, None),
            P("section", "tensor", "seq"),
            P("section", None),
            P("section", None),
            P("section", None),
            P("section", "seq", "tensor"),
            P("section", None),
            P("section", "tensor", "seq"),
            P("section", None),
        ),
        check_vma=False,
    )
```

```python
import functools
import types

import jax
import jax.numpy as jnp
from jax import lax
from jax.experimental import pallas as pl
from jax.experimental.pallas import tpu as pltpu
from jax.sharding import PartitionSpec as P

HDIM = 64
WIN = 64
QB = 64
KSEL = 64


NORM_EPS = 1e-05
MASKED = -1000000000.0


def from_behind(value, axis, steps):
    count = lax.axis_size(axis)
    first, last = (max(0, -steps), min(count, count - steps))
    return lax.ppermute(value, axis, [(source, source + steps) for source in range(first, last)])


def layer_norm(values, gain, shift):
    average = jnp.mean(values, axis=-1, keepdims=True)
    centred = values - average
    variance = jnp.mean(centred * centred, axis=-1, keepdims=True)
    return centred * lax.rsqrt(variance + NORM_EPS) * gain + shift


def gelu_tanh(values):
    return (
        0.5
        * values
        * (1.0 + jnp.tanh(0.7978845608028654 * (values + 0.044715 * values * values * values)))
    )


def gather_rows(row_block):
    return lax.all_gather(row_block, "tensor", axis=0, tiled=True)


def scatter_product(left_rows, weight, formula):
    return lax.psum_scatter(
        jnp.einsum(formula, left_rows, weight, preferred_element_type=jnp.float32).astype(
            jnp.bfloat16
        ),
        "tensor",
        scatter_dimension=0,
        tiled=True,
    ).astype(jnp.float32)


def near_slabs(full_rows, seq_start, seq_first, length_local):
    buckets = full_rows.shape[1]
    heads_local = full_rows.shape[2] // HDIM
    blocks = length_local // QB
    earlier = lax.dynamic_slice_in_dim(full_rows, jnp.maximum(seq_start - WIN, 0), WIN, 0)
    earlier = jnp.where(seq_first, jnp.zeros_like(earlier), earlier)
    local_part = lax.dynamic_slice_in_dim(full_rows, seq_start, length_local, 0)
    segment = jnp.concatenate([earlier, local_part], 0).reshape(
        length_local + WIN, buckets, heads_local, HDIM
    )
    return jnp.concatenate(
        [
            segment[offset_index * QB : offset_index * QB + length_local].reshape(
                blocks, QB, buckets, heads_local, HDIM
            )
            for offset_index in range(WIN // QB + 1)
        ],
        1,
    )


def far_rows(full_rows, flat_index):
    total_rows, buckets, feature_width = full_rows.shape
    heads_local = feature_width // HDIM
    return jnp.take(full_rows.reshape(total_rows * buckets * heads_local, HDIM), flat_index, axis=0)


def key_geometry(chosen_now, seq_start, blocks):
    buckets, heads_local = (chosen_now.shape[0], chosen_now.shape[1])
    bucket_ids = lax.broadcasted_iota(jnp.int32, chosen_now.shape, 0)
    head_ids = lax.broadcasted_iota(jnp.int32, chosen_now.shape, 1)
    flat_index = (chosen_now * buckets + bucket_ids) * heads_local + head_ids
    block_start = seq_start + QB * lax.broadcasted_iota(jnp.int32, (blocks, 1, 1), 0)
    query_ids = lax.broadcasted_iota(jnp.int32, (1, QB, 1), 1)
    key_ids = lax.broadcasted_iota(jnp.int32, (1, 1, WIN + QB), 2)
    distance = query_ids + WIN - key_ids
    near_ok = (distance >= 0) & (distance < WIN) & (block_start + key_ids - WIN >= 0)
    far_ok = chosen_now + WIN <= block_start.reshape(1, 1, blocks, 1)
    near_mask = jnp.broadcast_to(
        near_ok[:, None, None], (blocks, buckets, heads_local, QB, WIN + QB)
    )
    far_mask = jnp.broadcast_to(
        jnp.transpose(far_ok, (2, 0, 1, 3))[:, :, :, None, :],
        (blocks, buckets, heads_local, QB, KSEL),
    )
    return (flat_index, jnp.concatenate([near_mask, far_mask], -1))


def attention_setup(queries, key_rows, value_rows, chosen_now, seq_start, seq_first):
    length_local, buckets, feature_width = queries.shape
    heads_local = feature_width // HDIM
    blocks = length_local // QB
    query_blocks = queries.reshape(blocks, QB, buckets, heads_local, HDIM)
    flat_index, key_mask = key_geometry(chosen_now, seq_start, blocks)
    near_keys = near_slabs(key_rows, seq_start, seq_first, length_local)
    near_values = near_slabs(value_rows, seq_start, seq_first, length_local)
    far_keys = far_rows(key_rows, flat_index)
    far_values = far_rows(value_rows, flat_index)
    near_scores = jnp.einsum(
        "bqnhe,btnhe->bnhqt", query_blocks, near_keys, preferred_element_type=jnp.float32
    )
    far_scores = jnp.einsum(
        "bqnhe,nhbke->bnhqk", query_blocks, far_keys, preferred_element_type=jnp.float32
    )
    scores = jnp.where(
        key_mask, HDIM ** (-0.5) * jnp.concatenate([near_scores, far_scores], -1), MASKED
    )
    return (query_blocks, near_keys, near_values, far_keys, far_values, flat_index, scores)


def attend(queries, key_rows, value_rows, chosen_now, seq_start, seq_first):
    query_blocks, near_keys, near_values, far_keys, far_values, flat_index, scores = (
        attention_setup(queries, key_rows, value_rows, chosen_now, seq_start, seq_first)
    )
    span = WIN + QB
    row_top = jnp.max(scores, -1, keepdims=True)
    exp_terms = jnp.exp(scores - row_top)
    row_total = jnp.sum(exp_terms, -1, keepdims=True)
    softmax_low = (exp_terms / row_total).astype(jnp.bfloat16)
    near_part = jnp.einsum(
        "bnhqt,btnhe->bqnhe",
        softmax_low[..., :span],
        near_values,
        preferred_element_type=jnp.float32,
    )
    far_part = jnp.einsum(
        "bnhqk,nhbke->bqnhe",
        softmax_low[..., span:],
        far_values,
        preferred_element_type=jnp.float32,
    )
    return ((near_part + far_part).reshape(queries.shape), row_top + jnp.log(row_total))


def spread_back(near_grad, far_grad, flat_index, seq_start, seq_first, total_rows):
    blocks, span, buckets, heads_local, head_size = near_grad.shape
    length_local = blocks * QB
    feature_width = heads_local * head_size
    segment = jnp.zeros((length_local + WIN, buckets, heads_local, head_size), jnp.float32)
    for offset_index in range(WIN // QB + 1):
        piece = near_grad[:, offset_index * QB : (offset_index + 1) * QB].reshape(
            length_local, buckets, heads_local, head_size
        )
        segment = segment.at[offset_index * QB : offset_index * QB + length_local].add(piece)
    full_rows = jnp.zeros((total_rows * buckets * heads_local, head_size), jnp.float32)
    full_rows = full_rows.at[flat_index.reshape(-1)].add(far_grad.reshape(-1, head_size))
    full_rows = full_rows.reshape(total_rows, buckets, feature_width)
    local_part = segment[WIN:].reshape(length_local, buckets, feature_width)
    earlier = jnp.where(seq_first, 0.0, segment[:WIN].reshape(WIN, buckets, feature_width))
    full_rows = lax.dynamic_update_slice_in_dim(
        full_rows,
        lax.dynamic_slice_in_dim(full_rows, seq_start, length_local, 0) + local_part,
        seq_start,
        0,
    )
    earlier_start = jnp.maximum(seq_start - WIN, 0)
    full_rows = lax.dynamic_update_slice_in_dim(
        full_rows,
        lax.dynamic_slice_in_dim(full_rows, earlier_start, WIN, 0) + earlier,
        earlier_start,
        0,
    )
    return full_rows


def attend_back(
    queries, key_rows, value_rows, chosen_now, seq_start, seq_first, log_total, grad_mixed
):
    query_blocks, near_keys, near_values, far_keys, far_values, flat_index, scores = (
        attention_setup(queries, key_rows, value_rows, chosen_now, seq_start, seq_first)
    )
    span = WIN + QB
    score_scale = HDIM ** (-0.5)
    grad_blocks = grad_mixed.reshape(query_blocks.shape)
    weights_full = jnp.exp(scores - log_total)
    softmax_low = weights_full.astype(jnp.bfloat16)
    grad_near_weights = jnp.einsum(
        "bqnhe,btnhe->bnhqt", grad_blocks, near_values, preferred_element_type=jnp.float32
    )
    grad_far_weights = jnp.einsum(
        "bqnhe,nhbke->bnhqk", grad_blocks, far_values, preferred_element_type=jnp.float32
    )
    grad_weights = jnp.concatenate([grad_near_weights, grad_far_weights], -1)
    row_dot = jnp.sum(weights_full * grad_weights, -1, keepdims=True)
    grad_scores = (weights_full * (grad_weights - row_dot)).astype(jnp.bfloat16)
    grad_near, grad_far = (grad_scores[..., :span], grad_scores[..., span:])
    grad_queries = score_scale * (
        jnp.einsum("bnhqt,btnhe->bqnhe", grad_near, near_keys, preferred_element_type=jnp.float32)
        + jnp.einsum("bnhqk,nhbke->bqnhe", grad_far, far_keys, preferred_element_type=jnp.float32)
    )
    near_key_grad = score_scale * jnp.einsum(
        "bnhqt,bqnhe->btnhe", grad_near, query_blocks, preferred_element_type=jnp.float32
    )
    far_key_grad = score_scale * jnp.einsum(
        "bnhqk,bqnhe->nhbke", grad_far, query_blocks, preferred_element_type=jnp.float32
    )
    near_value_grad = jnp.einsum(
        "bnhqt,bqnhe->btnhe",
        softmax_low[..., :span],
        grad_blocks,
        preferred_element_type=jnp.float32,
    )
    far_value_grad = jnp.einsum(
        "bnhqk,bqnhe->nhbke",
        softmax_low[..., span:],
        grad_blocks,
        preferred_element_type=jnp.float32,
    )
    total_rows = key_rows.shape[0]
    key_grad = spread_back(
        near_key_grad, far_key_grad, flat_index, seq_start, seq_first, total_rows
    )
    value_grad = spread_back(
        near_value_grad, far_value_grad, flat_index, seq_start, seq_first, total_rows
    )
    return (grad_queries.reshape(queries.shape), key_grad, value_grad)


def forward_pass(hidden, params, chosen_now, query_mask, seq_start, seq_first, finish):
    (
        ln1_gain,
        ln1_shift,
        w_qkv,
        b_qv,
        w_out,
        b_out,
        ln2_gain,
        ln2_shift,
        w_fc,
        b_fc,
        w_proj,
        b_proj,
    ) = params
    hidden_wide = hidden.astype(jnp.float32)
    normed_all = gather_rows(layer_norm(hidden_wide, ln1_gain, ln1_shift).astype(jnp.bfloat16))
    projected = jnp.einsum("pnd,jdc->jpnc", normed_all, w_qkv, preferred_element_type=jnp.float32)
    queries = (projected[0] + b_qv[0]).astype(jnp.bfloat16)
    key_rows, value_rows = (
        lax.all_gather(projected[1].astype(jnp.bfloat16), "seq", axis=0, tiled=True),
        lax.all_gather((projected[2] + b_qv[1]).astype(jnp.bfloat16), "seq", axis=0, tiled=True),
    )
    attended, log_total = attend(queries, key_rows, value_rows, chosen_now, seq_start, seq_first)
    mixed_rows = (attended * query_mask[:, :, None]).astype(jnp.bfloat16)
    middle = hidden_wide + scatter_product(mixed_rows, w_out, "pnc,cd->pnd") + b_out
    normed_mlp = gather_rows(layer_norm(middle, ln2_gain, ln2_shift).astype(jnp.bfloat16))
    pre_active = (
        jnp.einsum("pnd,df->pnf", normed_mlp, w_fc, preferred_element_type=jnp.float32) + b_fc
    )
    active = gelu_tanh(pre_active).astype(jnp.bfloat16)
    if not finish:
        return (
            normed_all,
            queries,
            key_rows,
            value_rows,
            log_total,
            mixed_rows,
            middle,
            normed_mlp,
            pre_active,
            active,
        )
    output = (middle + scatter_product(active, w_proj, "pnf,fd->pnd") + b_proj).astype(jnp.bfloat16)
    return (output, (key_rows, value_rows))


def backward_pass(hidden, upstream, params, chosen_now, query_mask, seq_start, seq_first):
    (
        ln1_gain,
        ln1_shift,
        w_qkv,
        b_qv,
        w_out,
        b_out,
        ln2_gain,
        ln2_shift,
        w_fc,
        b_fc,
        w_proj,
        b_proj,
    ) = params
    (
        normed_all,
        queries,
        key_rows,
        value_rows,
        log_total,
        mixed_rows,
        middle,
        normed_mlp,
        pre_active,
        active,
    ) = forward_pass(hidden, params, chosen_now, query_mask, seq_start, seq_first, False)
    upstream_all = gather_rows(upstream)
    grad_w_proj = jnp.einsum(
        "pnf,pnd->fd", active, upstream_all, preferred_element_type=jnp.float32
    )
    grad_b_proj = jnp.sum(upstream.astype(jnp.float32), axis=(0, 1))
    grad_active = jnp.einsum(
        "pnd,fd->pnf", upstream_all, w_proj, preferred_element_type=jnp.float32
    )
    unused_value, gelu_pull = jax.vjp(gelu_tanh, pre_active)
    grad_pre = gelu_pull(grad_active)[0].astype(jnp.bfloat16)
    grad_w_fc = jnp.einsum("pnd,pnf->df", normed_mlp, grad_pre, preferred_element_type=jnp.float32)
    grad_b_fc = jnp.sum(grad_pre.astype(jnp.float32), axis=(0, 1))
    grad_normed_mlp = scatter_product(grad_pre, w_fc, "pnf,df->pnd")
    unused_norm, second_pull = jax.vjp(layer_norm, middle, ln2_gain, ln2_shift)
    grad_mid_norm, grad_ln2_gain, grad_ln2_shift = second_pull(grad_normed_mlp)
    grad_middle = upstream.astype(jnp.float32) + grad_mid_norm
    grad_branch = grad_middle.astype(jnp.bfloat16)
    grad_b_out = jnp.sum(grad_branch.astype(jnp.float32), axis=(0, 1))
    branch_all = gather_rows(grad_branch)
    grad_w_out = jnp.einsum(
        "pnc,pnd->cd", mixed_rows, branch_all, preferred_element_type=jnp.float32
    )
    grad_mixed = jnp.einsum(
        "pnd,cd->pnc", branch_all, w_out, preferred_element_type=jnp.float32
    ).astype(jnp.bfloat16) * query_mask[:, :, None].astype(jnp.bfloat16)
    grad_queries, key_grad_all, value_grad_all = attend_back(
        queries, key_rows, value_rows, chosen_now, seq_start, seq_first, log_total, grad_mixed
    )
    key_grad, value_grad = (
        lax.psum_scatter(
            key_grad_all.astype(jnp.bfloat16), "seq", scatter_dimension=0, tiled=True
        ).astype(jnp.float32),
        lax.psum_scatter(
            value_grad_all.astype(jnp.bfloat16), "seq", scatter_dimension=0, tiled=True
        ).astype(jnp.float32),
    )
    grad_project = jnp.stack(
        [
            grad_queries.astype(jnp.bfloat16),
            key_grad.astype(jnp.bfloat16),
            value_grad.astype(jnp.bfloat16),
        ],
        2,
    )
    grad_w_qkv = jnp.einsum(
        "pnd,pnjc->jdc", normed_all, grad_project, preferred_element_type=jnp.float32
    )
    grad_b_qv = jnp.sum(grad_project[:, :, 0::2].astype(jnp.float32), axis=(0, 1))
    grad_normed = scatter_product(grad_project, w_qkv, "pnjc,jdc->pnd")
    unused_first, first_pull = jax.vjp(layer_norm, hidden.astype(jnp.float32), ln1_gain, ln1_shift)
    grad_in_norm, grad_ln1_gain, grad_ln1_shift = first_pull(grad_normed)
    grad_hidden = (grad_middle + grad_in_norm).astype(jnp.bfloat16)
    block_grads = (
        grad_ln1_gain,
        grad_ln1_shift,
        grad_w_qkv,
        grad_b_qv,
        grad_w_out,
        grad_b_out,
        grad_ln2_gain,
        grad_ln2_shift,
        grad_w_fc,
        grad_b_fc,
        grad_w_proj,
        grad_b_proj,
    )
    return (grad_hidden, block_grads)


def on_device(
    inputs,
    cotangent,
    lengths,
    chosen,
    ln1_gain,
    ln1_shift,
    w_qkv,
    b_qv,
    w_out,
    b_out,
    ln2_gain,
    ln2_shift,
    w_fc,
    b_fc,
    w_proj,
    b_proj,
):
    params = tuple(
        (
            weight_array[0]
            for weight_array in (
                ln1_gain,
                ln1_shift,
                w_qkv,
                b_qv,
                w_out,
                b_out,
                ln2_gain,
                ln2_shift,
                w_fc,
                b_fc,
                w_proj,
                b_proj,
            )
        )
    )
    section_index = lax.axis_index("section")
    section_count = lax.axis_size("section")
    seq_index = lax.axis_index("seq")
    tensor_index = lax.axis_index("tensor")
    tensor_count = lax.axis_size("tensor")
    micro_count, rows_local, buckets, feature_width = inputs.shape
    length_local = rows_local * tensor_count
    heads_width = w_qkv.shape[-1]
    seq_start = seq_index * length_local
    seq_first = seq_index == 0
    positions = seq_start + lax.broadcasted_iota(jnp.int32, (micro_count, length_local, buckets), 1)
    mask_all = (positions < lengths[:, None, :]).astype(jnp.float32)
    mask_rows = lax.dynamic_slice_in_dim(mask_all, tensor_index * rows_local, rows_local, 1)
    step_count = micro_count + section_count - 1
    chosen_section = chosen[0]
    received = jnp.zeros((rows_local, buckets, feature_width), jnp.bfloat16)
    stored = jnp.zeros((micro_count, rows_local, buckets, feature_width), jnp.bfloat16)
    outputs = jnp.zeros_like(stored)
    for step_index in range(step_count):
        micro_index = step_index - section_index
        running = (micro_index >= 0) & (micro_index < micro_count)
        slot_index = jnp.clip(micro_index, 0, micro_count - 1)
        block_in = jnp.where(
            section_index == 0, lax.dynamic_index_in_dim(inputs, slot_index, 0, False), received
        )
        chosen_now = lax.dynamic_index_in_dim(chosen_section, slot_index, 0, False)
        query_mask = lax.dynamic_index_in_dim(mask_all, slot_index, 0, False)
        result, key_pair = forward_pass(
            block_in, params, chosen_now, query_mask, seq_start, seq_first, True
        )
        stored = jnp.where(
            running, lax.dynamic_update_index_in_dim(stored, block_in, slot_index, 0), stored
        )
        outputs = jnp.where(
            running, lax.dynamic_update_index_in_dim(outputs, result, slot_index, 0), outputs
        )
        received = from_behind(result, "section", 1)
    back_received = jnp.zeros((rows_local, buckets, feature_width), jnp.bfloat16)
    in_grads = jnp.zeros_like(stored)
    totals = None
    for step_index in range(step_count):
        micro_index = step_index - (section_count - 1 - section_index)
        running = (micro_index >= 0) & (micro_index < micro_count)
        slot_index = jnp.clip(micro_index, 0, micro_count - 1)
        chosen_now = lax.dynamic_index_in_dim(chosen_section, slot_index, 0, False)
        query_mask = lax.dynamic_index_in_dim(mask_all, slot_index, 0, False)
        local_mask = lax.dynamic_index_in_dim(mask_rows, slot_index, 0, False)
        top_grad = (
            lax.dynamic_index_in_dim(cotangent, slot_index, 0, False).astype(jnp.float32)
            * local_mask[:, :, None]
        ).astype(jnp.bfloat16)
        upstream = jnp.where(section_index == section_count - 1, top_grad, back_received)
        hidden = lax.dynamic_index_in_dim(stored, slot_index, 0, False)
        grad_hidden, block_grads = backward_pass(
            hidden, upstream, params, chosen_now, query_mask, seq_start, seq_first
        )
        block_grads = tuple(
            (jnp.where(running, grad_part, jnp.zeros_like(grad_part)) for grad_part in block_grads)
        )
        totals = (
            block_grads
            if step_index == 0
            else tuple(
                (total_part + grad_part for total_part, grad_part in zip(totals, block_grads))
            )
        )
        in_grads = jnp.where(
            running, lax.dynamic_update_index_in_dim(in_grads, grad_hidden, slot_index, 0), in_grads
        )
        back_received = from_behind(grad_hidden, "section", -1)
    (
        sum_ln1_gain,
        sum_ln1_shift,
        sum_w_qkv,
        sum_b_qv,
        sum_w_out,
        sum_b_out,
        sum_ln2_gain,
        sum_ln2_shift,
        sum_w_fc,
        sum_b_fc,
        sum_w_proj,
        sum_b_proj,
    ) = totals
    part_qkv, part_out, part_fc, part_proj = (
        lax.psum_scatter(
            sum_w_qkv.astype(jnp.bfloat16), "seq", scatter_dimension=1, tiled=True
        ).astype(jnp.float32),
        lax.psum_scatter(
            sum_w_out.astype(jnp.bfloat16), "seq", scatter_dimension=1, tiled=True
        ).astype(jnp.float32),
        lax.psum_scatter(
            sum_w_fc.astype(jnp.bfloat16), "seq", scatter_dimension=0, tiled=True
        ).astype(jnp.float32),
        lax.psum_scatter(
            sum_w_proj.astype(jnp.bfloat16), "seq", scatter_dimension=1, tiled=True
        ).astype(jnp.float32),
    )
    bias_qv = lax.dynamic_update_slice_in_dim(
        jnp.zeros((2, feature_width), jnp.float32), sum_b_qv, tensor_index * heads_width, 1
    )
    units_local = sum_b_fc.shape[0]
    bias_fc = lax.dynamic_update_slice_in_dim(
        jnp.zeros((units_local * tensor_count,), jnp.float32),
        sum_b_fc,
        tensor_index * units_local,
        0,
    )
    small_sums = lax.psum(
        (
            sum_ln1_gain,
            sum_ln1_shift,
            bias_qv,
            sum_b_out,
            sum_ln2_gain,
            sum_ln2_shift,
            bias_fc,
            sum_b_proj,
        ),
        ("seq", "tensor"),
    )
    return (
        outputs[None],
        in_grads[None],
        small_sums[0][None],
        small_sums[1][None],
        part_qkv[None],
        small_sums[2][None],
        part_out[None],
        small_sums[3][None],
        small_sums[4][None],
        small_sums[5][None],
        part_fc[None],
        small_sums[6][None],
        part_proj[None],
        small_sums[7][None],
    )


STREAMS = 4
NRM, NMLP, UPS, BRN, ACT, GPRE, MIX, DQKV = range(8)
F32 = jnp.float32
LOW = jnp.bfloat16
MESH_ID = pl.DeviceIdType.MESH


def dot_nn(left, right):
    return lax.dot_general(left, right, (((1,), (0,)), ((), ())), preferred_element_type=F32)


def dot_nt(left, right):
    return lax.dot_general(left, right, (((1,), (1,)), ((), ())), preferred_element_type=F32)


def dot_tn(left, right):
    return lax.dot_general(left, right, (((0,), (0,)), ((), ())), preferred_element_type=F32)


def standard(rows):
    centred = rows - jnp.mean(rows, axis=-1, keepdims=True)
    scale = lax.rsqrt(jnp.mean(centred * centred, axis=-1, keepdims=True) + NORM_EPS)
    return centred * scale, scale


def standard_back(grad, xhat, scale):
    inner = jnp.mean(grad * xhat, axis=-1, keepdims=True)
    return scale * (grad - jnp.mean(grad, axis=-1, keepdims=True) - xhat * inner)


def column_sum(rows):
    return jnp.sum(rows.astype(F32), axis=0, keepdims=True)


def relay_kernel(names, *refs):
    r = types.SimpleNamespace(**dict(zip(names, refs)))
    a, c, t = (lax.axis_index(name) for name in ("section", "seq", "tensor"))
    lines = lax.axis_size("section")
    chips = lax.axis_size("tensor")
    rows, buckets, width = r.inputs.shape[1:]
    half_width = width // 2
    local = rows * chips
    total = 2 * local
    stream_rows = local // STREAMS
    head_width = r.wo_in.shape[0]
    heads = head_width // HDIM
    blocks = local // QB
    units = r.wp_in.shape[0]
    scale = HDIM ** (-0.5)
    streams = range(STREAMS)

    def remote(src, dst, send, recv, **target):
        return pltpu.make_async_remote_copy(
            src_ref=src,
            dst_ref=dst,
            send_sem=send,
            recv_sem=recv,
            device_id=target,
            device_id_type=MESH_ID,
        )

    def drain(ref, sem):
        pltpu.make_async_copy(ref, ref, sem).wait()

    def row_block(index, size):
        return pl.ds(pl.multiple_of(index * size, size), size)

    near_chip = t + 1 - 2 * (t % 2)
    over_chip = (t + 2) % 4
    across_chip = 3 - t
    middle_chip = (t == 1) | (t == 2)
    end_chip = (t == 0) | (t == 3)
    owned = stream_rows // 2
    mine = row_block(t - 1, owned)
    my_half = row_block(c, local)

    barrier = pltpu.get_barrier_semaphore()
    for core in range(2):
        for step in range(1, chips):
            there = {"tensor": (t + step) % chips, "seq": core}
            pl.semaphore_signal(barrier, inc=1, device_id=there, device_id_type=MESH_ID)
        for step in range(1, lines):
            there = {"section": (a + step) % lines, "seq": core}
            pl.semaphore_signal(barrier, inc=1, device_id=there, device_id_type=MESH_ID)
    for step in range(1, lines):
        there = {"section": (a + step) % lines, "tensor": near_chip}
        pl.semaphore_signal(barrier, inc=1, device_id=there, device_id_type=MESH_ID)
    pl.semaphore_signal(barrier, inc=1, device_id={"seq": 1 - c}, device_id_type=MESH_ID)
    pl.semaphore_wait(barrier, 2 * (chips - 1) + 3 * (lines - 1) + 1)

    def route(s, core):
        beside, above = s + 1 - 2 * (s % 2), (s + 2) % 4
        return (s, beside, 3 - s, above) if core == 0 else (s, above, 3 - s, beside)

    def store(p):
        return (r.wq, r.wo, r.wf, r.wp)[p]

    def source(p):
        return (r.wq_in, r.wo_in, r.wf_in, r.wp_in)[p]

    FINE = ((0, 0, 2), (0, 1, 2), (1, 0, 1), (2, 0, 2), (2, 1, 2), (3, 0, 2), (3, 1, 2))
    COARSE = ((0, 0, 1), (1, 0, 1), (2, 0, 1), (3, 0, 1))
    ALL_FINE, ALL = range(7), range(4)

    def chunk_of(s, n):
        p, part, parts = (FINE if isinstance(s, int) and s == 0 else COARSE)[n]
        return p, part, parts, source(p).shape[0] // 2 // parts

    def half_view(s, n, core):
        p, part, parts, size = chunk_of(s, n)
        return store(p).at[s, row_block(core * parts + part, size)]

    def ring(s, n, target, first=False):
        p, part, parts, size = chunk_of(s, n)
        view = half_view(s, n, c)
        src = source(p).at[row_block(c * parts + part, size)] if first else view
        return remote(src, view, r.w_ring_s.at[s, n], r.w_ring_r.at[s, n], section=target)

    def core_hop(s, n, core):
        view = half_view(s, n, core)
        return remote(view, view, r.w_core_s.at[s, n], r.w_core_r.at[s, n], seq=1 - c)

    def own_copy(p):
        return pltpu.make_async_copy(source(p), store(p).at[a], r.w_own.at[p])

    def send(s, core, chunks):
        @pl.when((a == s) & (c == core))
        def _():
            for n in chunks:
                ring(s, n, route(s, core)[1], True).start()

    def take(s, core, hop, chunks):
        line = route(s, core)[hop]

        @pl.when((a == line) & (c == core))
        def _():
            for n in chunks:
                ring(s, n, line).wait_recv()
                if hop < 3:
                    ring(s, n, route(s, core)[hop + 1]).start()
                core_hop(s, n, c).start()

    def take_first(hop, chunks):
        for core in range(2):
            take(0, core, hop, chunks)

    def weights_at(section, point):
        Q, F, P = (0, 1, 2), (3, 4), (5, 6)
        q, o, f, p = range(4)
        if (section, point) == (0, 0):
            for hop in range(1, 4):
                take_first(hop, Q)
            take_first(1, F)
        if (section, point) == (0, 1):
            take_first(1, P)
            take_first(2, F)
        if (section, point) == (0, 2):
            take_first(2, P)
            take_first(3, F)
            send(1, 1, ALL)
        if (section, point) == (0, 3):
            take_first(3, P)
            take(1, 0, 2, (q, o))
            send(3, 1, ALL)
        if (section, point) == (0, 4):
            take(1, 0, 1, ALL)
            take(1, 1, 1, (q, o))
            take(1, 0, 2, (f,))
            take(2, 1, 1, ALL)
            send(2, 0, ALL)
        if (section, point) == (1, 0):
            take(1, 0, 3, (q, o))
            take(1, 1, 2, (q, o))
            take(1, 1, 3, (q, o))
        if (section, point) == (1, 1):
            take(1, 1, 1, (f, p))
            take(1, 0, 2, (p,))
            send(3, 0, ALL)
            take(2, 0, 1, (q,))
            take(2, 1, 2, ALL)
        if (section, point) == (1, 2):
            take(1, 0, 3, (f,))
            take(1, 1, 2, (f, p))
            take(1, 1, 3, (f,))
            take(2, 0, 1, (o,))
            take(3, 1, 1, (q, o, f))
        if (section, point) == (1, 3):
            take(1, 0, 3, (p,))
            take(1, 1, 3, (p,))
        if (section, point) == (1, 4):
            take(2, 0, 1, (f,))
            take(3, 0, 1, (q, o))
            take(3, 1, 1, (p,))
        if (section, point) == (2, 0):
            take(2, 0, 1, (p,))
            take(2, 0, 2, (q, o))
            take(2, 1, 3, (q, o))
            take(2, 0, 3, (q, o))
        if (section, point) == (2, 1):
            take(2, 0, 2, (f, p))
            take(3, 0, 1, (f, p))
            take(3, 1, 2, ALL)
        if (section, point) == (2, 4):
            take(3, 0, 2, (q, o, f))
        if (section, point) == (3, 0):
            take(3, 0, 2, (p,))
            take(3, 0, 3, (q, o))
            take(3, 1, 3, (q, o))
        if section in (2, 3) and point in (2, 3):
            take(section, 0, 3, (f if point == 2 else p,))
            take(section, 1, 3, (f if point == 2 else p,))

    def weights_point(s, point):
        for section in range(4):

            @pl.when(s == section)
            def _():
                weights_at(section, point)

    def need(s, p):
        @pl.when(a == s)
        def _():
            own_copy(p).wait()

        @pl.when((a != s) & (s == 0))
        def _():
            for n in ALL_FINE:
                if FINE[n][0] == p:
                    core_hop(0, n, 1 - c).wait_recv()

        @pl.when((a != s) & (s > 0))
        def _():
            core_hop(s, p, 1 - c).wait_recv()

    def small_copy(step, line, slot):
        return remote(
            r.small_own, r.small.at[slot], r.small_s.at[step], r.small_r.at[slot], section=line
        )

    def count_copy(step, line, slot):
        return remote(
            r.count_own.at[line],
            r.count.at[slot],
            r.count_s.at[step],
            r.count_r.at[slot],
            section=line,
        )

    singles = (r.ln1_gain, r.ln1_shift, r.ln2_gain, r.ln2_shift, r.b_out, r.b_proj)
    for place, single in enumerate(singles):
        r.small_own[place : place + 1] = single[...]
    r.small_own[6:7, :units] = r.b_fc[...]
    r.small_own[7:8, :head_width] = r.b_qv[0:1]
    r.small_own[7:8, half_width : half_width + head_width] = r.b_qv[1:2]
    for step in range(1, lines):
        small_copy(step - 1, (a + step) % lines, a).start()
    send(0, 0, ALL_FINE)
    send(0, 1, ALL_FINE)
    send(1, 0, ALL)
    send(2, 1, ALL)
    for p in range(4):
        own_copy(p).start()
    r.small[a] = r.small_own[...]

    def place_of(index):
        inside = index % local
        stream, left = inside // stream_rows, inside % stream_rows
        first = (index // local) * local + (left // owned) * (local // 2)
        return first + stream * owned + left % owned

    def iota(shape, dimension):
        return lax.broadcasted_iota(jnp.int32, shape, dimension)

    square = jnp.where(iota((KSEL, KSEL), 0) == iota((KSEL, KSEL), 1), 1.0, 0.0).astype(LOW)
    position = place_of(iota((KSEL, total), 1)).astype(F32)
    for pair in range(lines * heads):
        line, head = pair // heads, pair % heads
        columns = dot_nt(square, r.chosen[pair].astype(F32).astype(LOW))
        for block in range(blocks):
            pick = head * blocks + block
            r.count_own[line, pick : pick + 1, :] = jnp.sum(
                jnp.where(columns[:, block : block + 1] == position, 1.0, 0.0),
                axis=0,
                keepdims=True,
            )
    for step in range(1, lines):
        count_copy(step - 1, (a + step) % lines, a).start()
    r.count[a] = r.count_own[a]

    NEAR, OVER, ACROSS = range(3)

    def gather(buffer, s, kind, j, owner, target, slot):
        view = buffer.at[s, j, row_block(owner - 1, owned)]
        return remote(
            view, view, r.ag_s.at[kind, j, slot], r.ag_r.at[kind, j, slot], tensor=target
        )

    def gather_start(buffer, s, kind, j):
        gather(buffer, s, kind, j, t, over_chip, OVER).start()
        gather(buffer, s, kind, j, t, across_chip, ACROSS).start()
        gather(buffer, s, kind, j, t, near_chip, NEAR).start()

    def gather_wait(buffer, s, kind, j):
        @pl.when(middle_chip)
        def _():
            gather(buffer, s, kind, j, across_chip, across_chip, ACROSS).wait_recv()

        @pl.when(end_chip)
        def _():
            gather(buffer, s, kind, j, near_chip, near_chip, NEAR).wait_recv()
            gather(buffer, s, kind, j, over_chip, over_chip, OVER).wait_recv()

    def gather_sent(buffer, s, kind, j):
        @pl.when(middle_chip)
        def _():
            gather(buffer, s, kind, j, t, over_chip, OVER).wait_send()
            gather(buffer, s, kind, j, t, across_chip, ACROSS).wait_send()
            gather(buffer, s, kind, j, t, near_chip, NEAR).wait_send()

    def scatter(s, kind, j, owner, slot):
        return remote(
            r.part.at[kind, j, row_block(owner - 1, owned)],
            r.arrived.at[s, kind, j, slot],
            r.rs_s.at[kind, j, slot],
            r.rs_r.at[kind, j, slot],
            tensor=owner,
        )

    def scatter_start(s, kind, j, product):
        r.part[kind, j] = product.astype(LOW)

        @pl.when(end_chip)
        def _():
            scatter(s, kind, j, over_chip, OVER).start()
            scatter(s, kind, j, near_chip, NEAR).start()

        @pl.when(middle_chip)
        def _():
            scatter(s, kind, j, across_chip, ACROSS).start()

    def scatter_sum(s, kind, j):
        result = r.part[kind, j, mine].astype(F32)
        for slot in (NEAR, ACROSS, OVER):
            scatter(s, kind, j, t, slot).wait_recv()
            result = result + r.arrived[s, kind, j, slot].astype(F32)
        return result

    def scatter_sent(s, kind, j):
        @pl.when(end_chip)
        def _():
            scatter(s, kind, j, over_chip, OVER).wait_send()
            scatter(s, kind, j, near_chip, NEAR).wait_send()

        @pl.when(middle_chip)
        def _():
            scatter(s, kind, j, across_chip, ACROSS).wait_send()

    own_rows = (r.nrm, r.nmlp, r.ups, r.brn, r.act, r.gpre, r.mix, r.dqkv)
    all_rows = (
        r.all_nrm,
        r.all_nmlp,
        r.all_ups,
        r.all_brn,
        r.all_act,
        r.all_gpre,
        r.all_mix,
        r.all_dqkv,
    )

    def rows_copy(index, s, same, stays=False):
        core = c if same else 1 - c
        src = own_rows[index].at[s]
        dst = all_rows[index].at[a, c]
        if index <= BRN:
            src = src.at[:, :, row_block(core, half_width)]
        recv = r.rows_r.at[index]
        if stays:
            return pltpu.make_async_copy(src, dst, recv)
        if same:
            return remote(src, dst, r.rows_s.at[index, s, 0], recv, section=s)
        return remote(src, dst, r.rows_s.at[index, s, 1], recv, section=s, seq=1 - c)

    passed_rows = {UPS: r.pass_ups, GPRE: r.pass_gpre, BRN: r.pass_brn, DQKV: r.pass_dqkv}
    passer = (a == 1) & (c == 1)

    def detours(index, s):
        return (a == 3) & (c == 1) & (s == 0) if index in passed_rows else False

    def detour_copy(index):
        place = tuple(passed_rows).index(index)
        return remote(
            own_rows[index].at[0],
            passed_rows[index],
            r.pass_s.at[place],
            r.pass_r.at[place],
            section=1,
        )

    def pass_rows(index):
        @pl.when(passer)
        def _():
            detour_copy(index).wait_recv()
            passed_copies(index, lambda copy: copy.start())

    def passed_copies(index, act):
        place = tuple(passed_rows).index(index)
        for step in range(2 if index <= BRN else 1):
            core = (c + step) % 2
            src = passed_rows[index]
            if index <= BRN:
                src = src.at[:, :, row_block(core, half_width)]
            act(
                remote(
                    src,
                    all_rows[index].at[3, c],
                    r.pass_on_s.at[place, step],
                    r.rows_r.at[index],
                    section=0,
                    seq=core,
                )
            )

    def rows_start(index, s):
        @pl.when(a == s)
        def _():
            rows_copy(index, s, True, True).start()

        if index in passed_rows:

            @pl.when(detours(index, s))
            def _():
                detour_copy(index).start()

            sends = jnp.logical_not(detours(index, s))
        else:
            sends = True

        @pl.when((a != s) & sends)
        def _():
            rows_copy(index, s, True).start()

        if index <= BRN:

            @pl.when(sends)
            def _():
                rows_copy(index, s, False).start()

    def forward_rows(s):
        for index in (NRM, MIX, NMLP, ACT):
            rows_start(index, s)

    def rows_sent(index, s):
        if index in passed_rows:

            @pl.when(detours(index, s))
            def _():
                detour_copy(index).wait_send()

            @pl.when(passer & (s == 0))
            def _():
                passed_copies(index, lambda copy: copy.wait_send())

            sends = jnp.logical_not(detours(index, s))
        else:
            sends = True

        @pl.when((a != s) & sends)
        def _():
            rows_copy(index, s, True).wait_send()

        if index <= BRN:

            @pl.when(sends)
            def _():
                rows_copy(index, s, False).wait_send()

    def share_copy(index, core):
        view = all_rows[index].at[:, core]
        return remote(view, view, r.share_s.at[index - ACT], r.share_r.at[index - ACT], seq=1 - c)

    def share(index):
        drain(all_rows[index].at[:, c], r.rows_r.at[index])
        share_copy(index, c).start()

    def norm_copy(s):
        return remote(
            r.norm_part.at[s], r.norm_all.at[a], r.norm_s.at[s], r.norm_r, section=s
        )

    def norm_start(s):
        @pl.when(a == s)
        def _():
            pltpu.make_async_copy(r.norm_part.at[s], r.norm_all.at[a], r.norm_r).start()

        @pl.when(a != s)
        def _():
            norm_copy(s).start()

    def home_copy(what, s, chip):
        src, dst, send, recv = what
        return remote(
            src.at[s, chip % 2],
            dst.at[a],
            send.at[s, chip % 2],
            recv,
            section=s,
            tensor=chip,
        )

    def home_start(what, s):
        src, dst, send, recv = what

        @pl.when(middle_chip & (a == s))
        def _():
            pltpu.make_async_copy(src.at[s, t % 2], dst.at[a], recv).start()

        @pl.when(middle_chip & (a != s))
        def _():
            home_copy(what, s, t).start()

        @pl.when(middle_chip)
        def _():
            home_copy(what, s, near_chip).start()

    def home_sent(what, s):
        @pl.when(middle_chip & (a != s))
        def _():
            home_copy(what, s, t).wait_send()

        @pl.when(middle_chip)
        def _():
            home_copy(what, s, near_chip).wait_send()

    out_home = (r.out_low, r.acts, r.out_s, r.out_r)
    grad_home = (r.grad_low, r.grads, r.grad_s, r.grad_r)

    length = r.lengths[a // buckets, a % buckets]
    key = place_of(iota((stream_rows, total), 1))
    for j in streams:
        query = place_of(c * local + j * stream_rows + iota((stream_rows, total), 0))
        r.near[j] = jnp.where((query >= key) & (query - key < WIN), 1.0, 0.0)
    key_row = place_of(iota((1, total), 1))

    def row_mask(place):
        return jnp.where(place < length, 1.0, 0.0)

    def multiplicity(s, j, head):
        far = []
        for block in range(blocks):
            pick = head * blocks + block
            limit = (c * blocks + block) * QB - WIN
            counted = jnp.where(key_row <= limit, r.count[s, pick : pick + 1, :], 0.0)
            far.append(jnp.broadcast_to(counted, (stream_rows // blocks, total)))
        return r.near[j] + jnp.concatenate(far, axis=0)

    def head_cols(head):
        return slice(head * HDIM, (head + 1) * HDIM)

    def kv_copy(s):
        view = r.kv.at[s, :, 0:local]
        return remote(view, view, r.kv_s.at[s], r.kv_r.at[s], seq=1 - c)

    def dkv_copy(s):
        return remote(r.dkv_out.at[s], r.dkv_in.at[s], r.dkv_s.at[s], r.dkv_r.at[s], seq=1 - c)

    def own_sequence(ref):
        both = ref[a // buckets].astype(F32)
        picked = both[:, 0, :]
        for bucket in range(1, buckets):
            picked = jnp.where(a % buckets == bucket, both[:, bucket, :], picked)
        return picked

    def own_part(j):
        chip, first = (j * owned) // rows, (j * owned) % rows
        return chip, slice(first, first + owned)

    def first_copy():
        return remote(r.first_out, r.first_in, r.first_s, r.first_r, tensor=near_chip)

    own_place = c * local + t * rows + iota((rows, 1), 0)
    r.first_out[0] = own_sequence(r.inputs).astype(LOW)
    r.first_out[1] = (own_sequence(r.cotangent) * row_mask(own_place)).astype(LOW)
    r.norm_part[...] = jnp.zeros_like(r.norm_part)

    @pl.when(c == 0)
    def _():
        r.kv[:, :, local:total] = jnp.zeros((lines, 2, local, head_width), LOW)


    @pl.when(end_chip)
    def _():
        first_copy().start()

    @pl.when(middle_chip)
    def _():
        first_copy().wait_recv()
        for which in range(2):
            here, beside_it = r.first_out[which].astype(F32), r.first_in[which].astype(F32)
            lower = jnp.where(t % 2 == 0, here, beside_it)
            upper = jnp.where(t % 2 == 0, beside_it, here)
            for j in streams:
                chip, part = own_part(j)
                own_block = (lower, upper)[chip][part]
                if which == 0:
                    r.hidden[j] = own_block
                else:
                    r.upstream[j] = own_block.astype(LOW)

    def on_owner(stage):
        def run(s, j):
            @pl.when(middle_chip)
            def _():
                stage(s, j)

        return run

    def keep_rows(target, s, j, result):
        chip, part = own_part(j)
        target[s, chip, part] = result

    @on_owner
    def enter(s, j):
        xhat, inverse = standard(r.hidden[j])
        r.xhat1[s, j] = xhat
        r.inv1[s, j] = jnp.broadcast_to(inverse, (owned, 128))
        r.nrm[s, j, mine] = (xhat * r.small[s, 0:1] + r.small[s, 1:2]).astype(LOW)
        gather_start(r.nrm, s, 0, j)

    def project(s, j):
        gather_wait(r.nrm, s, 0, j)
        normed = r.nrm[s, j]
        place = row_block(c * STREAMS + j, stream_rows)
        bias_v = r.small[s, 7:8, half_width : half_width + head_width]
        key_rows = dot_nt(normed, r.wq[s, head_width : 2 * head_width])
        value_rows = dot_nt(normed, r.wq[s, 2 * head_width : 3 * head_width]) + bias_v
        r.kv[s, 0, place] = key_rows.astype(LOW)
        r.kv[s, 1, place] = value_rows.astype(LOW)
        gather_sent(r.nrm, s, 0, j)

    def ask(s, j):
        queries = dot_nt(r.nrm[s, j], r.wq[s, 0:head_width]) + r.small[s, 7:8, :head_width]
        r.qry[s, j] = queries.astype(LOW)

    def attend_line(s, j):
        mixed = []
        for head in range(heads):
            cols = head_cols(head)
            times = multiplicity(s, j, head)
            scores = scale * dot_nt(r.qry[s, j, :, cols], r.kv[s, 0, :, cols])
            scores = jnp.where(times > 0.0, scores, MASKED)
            top = jnp.max(scores, axis=-1, keepdims=True)
            terms = times * jnp.exp(scores - top)
            weights = terms / jnp.sum(terms, axis=-1, keepdims=True)
            r.soft[s, j, head] = weights
            mixed.append(dot_nn(weights.astype(LOW), r.kv[s, 1, :, cols]))
        mask = row_mask(place_of(c * local + j * stream_rows + iota((stream_rows, 1), 0)))
        r.mix[s, j] = (jnp.concatenate(mixed, axis=-1) * mask).astype(LOW)

    def leave_attention(s, j):
        scatter_start(s, 0, j, dot_nn(r.mix[s, j], r.wo[s]))

    @on_owner
    def between(s, j):
        middle = r.hidden[j] + scatter_sum(s, 0, j) + r.small[s, 4:5]
        r.middle[j] = middle
        xhat, inverse = standard(middle)
        r.xhat2[s, j] = xhat
        r.inv2[s, j] = jnp.broadcast_to(inverse, (owned, 128))
        r.nmlp[s, j, mine] = (xhat * r.small[s, 2:3] + r.small[s, 3:4]).astype(LOW)
        gather_start(r.nmlp, s, 1, j)

    def feed(s, j):
        gather_wait(r.nmlp, s, 1, j)
        before = dot_nn(r.nmlp[s, j], r.wf[s]) + r.small[s, 6:7, :units]
        bend = jnp.tanh(0.7978845608028654 * (before + 0.044715 * before * before * before))
        r.act[s, j] = (0.5 * before * (1.0 + bend)).astype(LOW)
        r.slope[s, j] = 0.5 * (1.0 + bend) + 0.5 * before * (1.0 - bend * bend) * (
            0.7978845608028654 * (1.0 + 3 * 0.044715 * before * before)
        )

        gather_sent(r.nmlp, s, 1, j)

    def leave_feed(s, j):
        scatter_start(s, 1, j, dot_nn(r.act[s, j], r.wp[s]))

    @on_owner
    def finish(s, j):
        result = r.middle[j] + scatter_sum(s, 1, j) + r.small[s, 5:6]
        keep_rows(r.out_low, s, j, result.astype(LOW))
        r.hidden[j] = result.astype(LOW).astype(F32)

    def small_ready(s):
        @pl.when(a != s)
        def _():
            small_copy(0, a, s).wait_recv()

    small_ready(0)
    for j in streams:
        enter(0, j)

    def forward(s, _):
        weights_point(s, 0)
        need(s, 0)
        for j in streams:
            project(s, j)

        @pl.when(c == 0)
        def _():
            kv_copy(s).start()

        for j in streams:
            ask(s, j)

        @pl.when(a != s)
        def _():
            count_copy(0, a, s).wait_recv()

        @pl.when(c == 1)
        def _():
            kv_copy(s).wait_recv()

        for j in streams:
            attend_line(s, j)
            if j == 0:
                need(s, 1)
            leave_attention(s, j)

        weights_point(s, 1)
        for j in streams:
            between(s, j)
            scatter_sent(s, 0, j)
        weights_point(s, 2)
        need(s, 2)
        for j in streams:
            feed(s, j)
            if j == 0:
                weights_point(s, 3)
                need(s, 3)
            leave_feed(s, j)


        @pl.when(s >= 2)
        def _():
            forward_rows(s - 2)


        @pl.when(s + 1 < lines)
        def _():
            small_ready(s + 1)

        for j in streams:
            finish(s, j)
            scatter_sent(s, 1, j)

            @pl.when(s + 1 < lines)
            def _():
                enter(s + 1, j)

        home_start(out_home, s)

        weights_point(s, 4)
        return 0

    lax.fori_loop(0, lines, forward, 0)

    @on_owner
    def turn(s, j):
        upstream = r.upstream[j]
        r.ups[s, j, mine] = upstream
        gather_start(r.ups, s, 2, j)
        r.norm_part[s, 5:6] += column_sum(upstream)

    def feed_back(s, j):
        gather_wait(r.ups, s, 2, j)
        grad_pre = (dot_nt(r.ups[s, j], r.wp[s]) * r.slope[s, j]).astype(LOW)
        r.gpre[s, j] = grad_pre
        scatter_start(s, 2, j, dot_nt(grad_pre, r.wf[s]))
        r.norm_part[s, 6:7, :units] += column_sum(grad_pre)
        gather_sent(r.ups, s, 2, j)

    @on_owner
    def between_back(s, j):
        grad = scatter_sum(s, 2, j)
        xhat = r.xhat2[s, j]
        upstream = r.upstream[j].astype(F32)
        grad_middle = upstream + standard_back(
            grad * r.small[s, 2:3], xhat, r.inv2[s, j, :, 0:1]
        )
        r.middle[j] = grad_middle
        branch = grad_middle.astype(LOW)
        r.brn[s, j, mine] = branch
        gather_start(r.brn, s, 3, j)
        r.norm_part[s, 2:3] += column_sum(grad * xhat)
        r.norm_part[s, 3:4] += column_sum(grad)
        r.norm_part[s, 4:5] += column_sum(branch)

    def mixed_back(s, j):
        gather_wait(r.brn, s, 3, j)
        place = place_of(c * local + j * stream_rows + iota((stream_rows, 1), 0))
        r.gmix[j] = (dot_nt(r.brn[s, j], r.wo[s]) * row_mask(place)).astype(LOW)
        gather_sent(r.brn, s, 3, j)

    def attend_line_back(s, j):
        grad_q, grad_k, grad_v = [], [], []
        for head in range(heads):
            cols = head_cols(head)
            weights = r.soft[s, j, head]
            grad_head = r.gmix[j, :, cols]
            grad_weights = dot_nt(grad_head, r.kv[s, 1, :, cols])
            inner = jnp.sum(weights * grad_weights, axis=-1, keepdims=True)
            grad_scores = (weights * (grad_weights - inner)).astype(LOW)
            grad_k.append(scale * dot_tn(grad_scores, r.qry[s, j, :, cols]))
            grad_v.append(dot_tn(weights.astype(LOW), grad_head))
            grad_q.append(scale * dot_nn(grad_scores, r.kv[s, 0, :, cols]))
        for which, grad in enumerate((grad_k, grad_v)):
            grad = jnp.concatenate(grad, axis=-1)
            r.dkv_all[which] = grad if j == 0 else r.dkv_all[which] + grad
        grad_q = jnp.concatenate(grad_q, axis=-1).astype(LOW)
        r.dqkv[s, 0, j] = grad_q
        r.norm_part[s, 7:8, :head_width] += column_sum(grad_q)

    def join_keys(s):
        @pl.when(c == 1)
        def _():
            r.dkv_out[s] = r.dkv_all[:, 0:local].astype(LOW)
            dkv_copy(s).start()

        @pl.when(c == 0)
        def _():
            dkv_copy(s).wait_recv()
            r.dkv_all[:, 0:local] += r.dkv_in[s].astype(F32)

        for which in range(2):
            joined = r.dkv_all[which, my_half].astype(LOW)
            r.dqkv[s, 1 + which] = joined.reshape(r.dqkv.shape[2:])
            if which == 1:
                r.norm_part[s, 7:8, half_width : half_width + head_width] = column_sum(joined)

    def leave_back(s, j):
        product = dot_nn(r.dqkv[s, 0, j], r.wq[s, 0:head_width])
        for which in range(1, 3):
            weight = r.wq[s, which * head_width : (which + 1) * head_width]
            product = product + dot_nn(r.dqkv[s, which, j], weight)
        scatter_start(s, 3, j, product)

    @on_owner
    def finish_back(s, j):
        grad = scatter_sum(s, 3, j)
        xhat = r.xhat1[s, j]
        result = r.middle[j] + standard_back(
            grad * r.small[s, 0:1], xhat, r.inv1[s, j, :, 0:1]
        )
        r.upstream[j] = result.astype(LOW)
        keep_rows(r.grad_low, s, j, result.astype(LOW))
        r.norm_part[s, 0:1] += column_sum(grad * xhat)
        r.norm_part[s, 1:2] += column_sum(grad)

    for j in streams:
        turn(lines - 1, j)

    def backward(index, _):
        s = lines - 1 - index
        for j in streams:
            feed_back(s, j)
        rows_start(UPS, s)
        rows_start(GPRE, s)

        @pl.when(index < 2)
        def _():
            forward_rows(lines - 2 + index)

        @pl.when(index == lines - 1)
        def _():
            share(ACT)
            share(MIX)

        for j in streams:
            between_back(s, j)
            scatter_sent(s, 2, j)
        for j in streams:
            mixed_back(s, j)
            attend_line_back(s, j)
        join_keys(s)
        rows_start(BRN, s)

        @pl.when(s == 0)
        def _():
            pass_rows(UPS)
            pass_rows(GPRE)

        for j in streams:
            leave_back(s, j)
        rows_start(DQKV, s)
        for j in streams:
            finish_back(s, j)
            scatter_sent(s, 3, j)

            @pl.when(s > 0)
            def _():
                turn(s - 1, j)

        norm_start(s)
        home_start(grad_home, s)
        return 0

    lax.fori_loop(0, lines, backward, 0)

    pass_rows(BRN)
    pass_rows(DQKV)
    share(GPRE)
    share(DQKV)

    drain(r.norm_all, r.norm_r)
    slot = c * chips + t
    norm_sum = r.norm_all[0]
    for line in range(1, lines):
        norm_sum = norm_sum + r.norm_all[line]
    r.ends[slot] = norm_sum

    def ends_copy(step):
        core, chip = step // chips, step % chips
        view = r.ends.at[slot]
        return remote(
            view,
            view,
            r.ends_s.at[step - 1],
            r.ends_r,
            seq=(c + core) % 2,
            tensor=(t + chip) % chips,
        )

    for step in range(1, 2 * chips):
        ends_copy(step).start()

    for index in range(ACT):
        drain(all_rows[index], r.rows_r.at[index])
    for index in range(ACT, 8):
        share_copy(index, 1 - c).wait_recv()
        share_copy(index, c).wait_send()
    drain(r.acts, r.out_r)
    drain(r.grads, r.grad_r)
    drain(r.ends.at[0 : 2 * chips - 1], r.ends_r)
    for step in range(1, 2 * chips):
        ends_copy(step).wait_send()
    for step in range(1, lines):
        small_copy(step - 1, (a + step) % lines, a).wait_send()
        count_copy(step - 1, (a + step) % lines, a).wait_send()
    for s in range(lines):
        chunks = ALL_FINE if s == 0 else ALL
        for core in range(2):

            @pl.when((c == core) & (a != route(s, core)[3]))
            def _():
                for n in chunks:
                    ring(s, n, route(s, core)[1]).wait_send()

        @pl.when(a != s)
        def _():
            for n in chunks:
                core_hop(s, n, c).wait_send()

    @pl.when(end_chip)
    def _():
        first_copy().wait_send()

    def sent(s, _):
        home_sent(out_home, s)
        home_sent(grad_home, s)

        @pl.when(a != s)
        def _():
            norm_copy(s).wait_send()

        @pl.when(c == 0)
        def _():
            kv_copy(s).wait_send()

        @pl.when(c == 1)
        def _():
            dkv_copy(s).wait_send()

        for index in range(8):
            rows_sent(index, s)
        return 0

    lax.fori_loop(0, lines, sent, 0)


def relay_call(inputs, cotangent, lengths, chosen, singles, weights):
    lines = lax.axis_size("section")
    chips = lax.axis_size("tensor")
    rows, buckets, width = inputs.shape[1:]
    local, total, half = rows * chips, 2 * rows * chips, width // 2
    head_width, units = weights["wo_in"].shape[0], weights["wp_in"].shape[0]
    heads = head_width // HDIM
    stream = local // STREAMS
    peers, owned = chips - 1, stream // 2
    vmem, dma = pltpu.VMEM, pltpu.SemaphoreType.DMA
    operands = dict(
        inputs=inputs,
        cotangent=cotangent,
        lengths=lengths,
        chosen=chosen,
        **singles,
        **weights,
    )

    def space(name):
        if name in weights:
            return pl.ANY
        return pltpu.SMEM if operands[name] is lengths else pltpu.VMEM

    sums = dict(
        acts=((lines, rows, width), LOW),
        grads=((lines, rows, width), LOW),
        ends=((2 * chips, 8, width), F32),
    )
    gathered = dict(
        all_nrm=((lines, 2, STREAMS, stream, half), LOW),
        all_nmlp=((lines, 2, STREAMS, stream, half), LOW),
        all_ups=((lines, 2, STREAMS, stream, half), LOW),
        all_brn=((lines, 2, STREAMS, stream, half), LOW),
        all_act=((lines, 2, STREAMS, stream, units), LOW),
        all_gpre=((lines, 2, STREAMS, stream, units), LOW),
        all_mix=((lines, 2, STREAMS, stream, head_width), LOW),
        all_dqkv=((lines, 2, 3, STREAMS, stream, head_width), LOW),
    )
    outputs = dict(**sums, **gathered)
    scratch = dict(
        wq=vmem((lines,) + weights["wq_in"].shape, LOW),
        wo=vmem((lines,) + weights["wo_in"].shape, LOW),
        wf=vmem((lines,) + weights["wf_in"].shape, LOW),
        wp=vmem((lines,) + weights["wp_in"].shape, LOW),
        small_own=vmem((8, width), F32),
        small=vmem((lines, 8, width), F32),
        count_own=vmem((lines, 8, total), F32),
        count=vmem((lines, 8, total), F32),
        hidden=vmem((STREAMS, owned, width), F32),
        middle=vmem((STREAMS, owned, width), F32),
        upstream=vmem((STREAMS, owned, width), LOW),
        first_out=vmem((2, rows, width), LOW),
        first_in=vmem((2, rows, width), LOW),
        xhat1=vmem((lines, STREAMS, owned, width), F32),
        inv1=vmem((lines, STREAMS, owned, 128), F32),
        xhat2=vmem((lines, STREAMS, owned, width), F32),
        inv2=vmem((lines, STREAMS, owned, 128), F32),
        nrm=vmem((lines, STREAMS, stream, width), LOW),
        nmlp=vmem((lines, STREAMS, stream, width), LOW),
        ups=vmem((lines, STREAMS, stream, width), LOW),
        brn=vmem((lines, STREAMS, stream, width), LOW),
        act=vmem((lines, STREAMS, stream, units), LOW),
        gpre=vmem((lines, STREAMS, stream, units), LOW),
        slope=vmem((lines, STREAMS, stream, units), F32),
        mix=vmem((lines, STREAMS, stream, head_width), LOW),
        qry=vmem((lines, STREAMS, stream, head_width), LOW),
        gmix=vmem((STREAMS, stream, head_width), LOW),
        dqkv=vmem((lines, 3, STREAMS, stream, head_width), LOW),
        pass_ups=vmem((STREAMS, stream, width), LOW),
        pass_gpre=vmem((STREAMS, stream, units), LOW),
        pass_brn=vmem((STREAMS, stream, width), LOW),
        pass_dqkv=vmem((3, STREAMS, stream, head_width), LOW),
        kv=vmem((lines, 2, total, head_width), LOW),
        soft=vmem((lines, STREAMS, heads, stream, total), F32),
        near=vmem((STREAMS, stream, total), F32),
        dkv_all=vmem((2, total, head_width), F32),
        dkv_out=vmem((lines, 2, local, head_width), LOW),
        dkv_in=vmem((lines, 2, local, head_width), LOW),
        part=vmem((4, STREAMS, stream, width), LOW),
        arrived=vmem((lines, 4, STREAMS, peers, owned, width), LOW),
        out_low=vmem((lines, 2, rows, width), LOW),
        grad_low=vmem((lines, 2, rows, width), LOW),
        norm_part=vmem((lines, 8, width), F32),
        norm_all=vmem((lines, 8, width), F32),
        w_ring_s=dma((lines, 7)),
        w_ring_r=dma((lines, 7)),
        w_core_s=dma((lines, 7)),
        w_core_r=dma((lines, 7)),
        w_own=dma((4,)),
        small_s=dma((lines - 1,)),
        small_r=dma((lines,)),
        count_s=dma((lines - 1,)),
        count_r=dma((lines,)),
        ag_s=dma((4, STREAMS, peers)),
        ag_r=dma((4, STREAMS, peers)),
        rs_s=dma((4, STREAMS, peers)),
        rs_r=dma((4, STREAMS, peers)),
        kv_s=dma((lines,)),
        kv_r=dma((lines,)),
        dkv_s=dma((lines,)),
        dkv_r=dma((lines,)),
        rows_s=dma((8, lines, 2)),
        rows_r=dma((8,)),
        pass_s=dma((4,)),
        pass_r=dma((4,)),
        pass_on_s=dma((4, 2)),
        share_s=dma((4,)),
        share_r=dma((4,)),
        first_s=dma,
        first_r=dma,
        out_s=dma((lines, 2)),
        out_r=dma,
        grad_s=dma((lines, 2)),
        grad_r=dma,
        norm_s=dma((lines,)),
        norm_r=dma,
        ends_s=dma((2 * chips - 1,)),
        ends_r=dma,
    )
    names = tuple(operands) + tuple(outputs) + tuple(scratch)
    results = pl.pallas_call(
        functools.partial(relay_kernel, names),
        out_shape=[jax.ShapeDtypeStruct(shape, kind) for shape, kind in outputs.values()],
        in_specs=[pl.BlockSpec(memory_space=space(name)) for name in operands],
        out_specs=[
            pl.BlockSpec(memory_space=pl.ANY if name in gathered else pltpu.VMEM)
            for name in outputs
        ],
        scratch_shapes=list(scratch.values()),
        compiler_params=pltpu.CompilerParams(
            collective_id=0, has_side_effects=True, vmem_limit_bytes=60 * 2**20
        ),
        name="relay",
    )(*operands.values())
    return dict(zip(outputs, results))


def weights_kernel(names, *refs):
    r = types.SimpleNamespace(**dict(zip(names, refs)))
    step = pl.program_id(0)
    micro_count, rows, buckets, width = r.activations.shape
    chips, units, head_width = r.ends.shape[0] // 2, r.all_act.shape[-1], r.all_mix.shape[-1]

    @pl.when(step == 0)
    def _():
        sums = r.ends[0]
        for other in range(1, 2 * chips):
            sums = sums + r.ends[other]
        singles = (r.ln1_gain, r.ln1_shift, r.ln2_gain, r.ln2_shift, r.b_out, r.b_proj)
        for place, single in enumerate(singles):
            single[...] = sums[place : place + 1]
        for chip in range(chips):
            both = r.ends[chip] + r.ends[chips + chip]
            r.b_fc[:, chip * units : (chip + 1) * units] = both[6:7, :units]
            here = slice(chip * head_width, (chip + 1) * head_width)
            r.b_qv[0:1, here] = both[7:8, :head_width]
            r.b_qv[1:2, here] = both[7:8, width // 2 : width // 2 + head_width]
        for target, source in ((r.activations, r.acts), (r.in_grads, r.grads)):
            for micro in range(micro_count):
                rows_of = [
                    source[micro * buckets + bucket].astype(F32)[:, None, :]
                    for bucket in range(buckets)
                ]
                target[micro] = jnp.concatenate(rows_of, axis=1).astype(LOW)
        for target in (r.w_qkv, r.w_out, r.w_fc, r.w_proj):
            target[...] = jnp.zeros_like(target)

    def rows_of_sequence(ref):
        return ref[0].reshape(2 * chips * rows, ref.shape[-1])

    nrm, nmlp, ups, brn, act, gpre, mix = (
        rows_of_sequence(ref)
        for ref in (r.all_nrm, r.all_nmlp, r.all_ups, r.all_brn, r.all_act, r.all_gpre, r.all_mix)
    )
    r.w_proj[...] += dot_tn(act, ups)
    r.w_fc[...] += dot_tn(nmlp, gpre)
    r.w_out[...] += dot_tn(mix, brn)
    for which in range(3):
        grad = r.all_dqkv[0, :, which].reshape(2 * chips * rows, head_width)
        r.w_qkv[which] += dot_tn(grad, nrm)


def weights_call(relayed, inputs_shape, head_width, units):
    lines = lax.axis_size("section")
    chips = lax.axis_size("tensor")
    width = inputs_shape[-1]
    half = width // 2
    outputs = dict(
        activations=(inputs_shape, LOW),
        in_grads=(inputs_shape, LOW),
        ln1_gain=((1, width), F32),
        ln1_shift=((1, width), F32),
        w_qkv=((3, head_width, half), F32),
        b_qv=((2, width), F32),
        w_out=((head_width, half), F32),
        b_out=((1, width), F32),
        ln2_gain=((1, width), F32),
        ln2_shift=((1, width), F32),
        w_fc=((half, units), F32),
        b_fc=((1, chips * units), F32),
        w_proj=((units, half), F32),
        b_proj=((1, width), F32),
    )

    def spec(array):
        if len(array.shape) < 5:
            return pl.BlockSpec(array.shape, lambda step: (0,) * len(array.shape))
        return pl.BlockSpec(
            (1,) + array.shape[1:], lambda step: (step,) + (0,) * (len(array.shape) - 1)
        )

    def whole(shape):
        return pl.BlockSpec(shape, lambda step: (0,) * len(shape))

    return pl.pallas_call(
        functools.partial(weights_kernel, tuple(relayed) + tuple(outputs)),
        out_shape=[jax.ShapeDtypeStruct(shape, kind) for shape, kind in outputs.values()],
        grid=(lines,),
        in_specs=[spec(array) for array in relayed.values()],
        out_specs=[whole(shape) for shape, _ in outputs.values()],
        compiler_params=pltpu.CompilerParams(vmem_limit_bytes=60 * 2**20),
        name="weight_gradients",
    )(*relayed.values())


def on_line(
    inputs,
    cotangent,
    lengths,
    chosen,
    ln1_gain,
    ln1_shift,
    w_qkv,
    b_qv,
    w_out,
    b_out,
    ln2_gain,
    ln2_shift,
    w_fc,
    b_fc,
    w_proj,
    b_proj,
):
    head_width, units = w_out.shape[1], w_fc.shape[2]
    singles = dict(
        ln1_gain=ln1_gain,
        ln1_shift=ln1_shift,
        ln2_gain=ln2_gain,
        ln2_shift=ln2_shift,
        b_out=b_out,
        b_proj=b_proj,
        b_fc=b_fc,
        b_qv=b_qv[0],
    )
    weights = dict(
        wq_in=jnp.swapaxes(w_qkv[0], 1, 2).reshape(-1, inputs.shape[-1]),
        wo_in=w_out[0],
        wf_in=w_fc[0],
        wp_in=w_proj[0],
    )
    picks = chosen.reshape((-1,) + chosen.shape[-2:])
    relayed = relay_call(inputs, cotangent, lengths, picks, singles, weights)
    results = list(weights_call(relayed, inputs.shape, head_width, units))
    results[4] = jnp.swapaxes(results[4], 1, 2)
    vectors = (2, 3, 7, 8, 9, 11, 13)
    return tuple(
        result if place in vectors else result[None] for place, result in enumerate(results)
    )


def fits_lines(mesh):
    return mesh.shape["section"] == 4 and mesh.shape["seq"] == 2 and mesh.shape["tensor"] == 4


def solution(mesh):
    placed = (
        P(None, ("seq", "tensor"), None, None),
        P(None, ("seq", "tensor"), None, None),
        P(),
        P("section", None, None, "tensor", "seq", None),
        P("section", None),
        P("section", None),
        P("section", None, None, "tensor"),
        P("section", None, "tensor"),
        P("section", "tensor", None),
        P("section", None),
        P("section", None),
        P("section", None),
        P("section", None, "tensor"),
        P("section", "tensor"),
        P("section", "tensor", None),
        P("section", None),
    )
    return jax.shard_map(
        on_line if fits_lines(mesh) else on_device,
        mesh=mesh,
        in_specs=placed,
        out_specs=(
            P("section", None, ("seq", "tensor"), None, None),
            P("section", None, ("seq", "tensor"), None, None),
            P("section", None),
            P("section", None),
            P("section", None, "seq", "tensor"),
            P("section", None, None),
            P("section", "tensor", "seq"),
            P("section", None),
            P("section", None),
            P("section", None),
            P("section", "seq", "tensor"),
            P("section", None),
            P("section", "tensor", "seq"),
            P("section", None),
        ),
        check_vma=False,
    )
```

```python
import functools
import types

import jax
import jax.numpy as jnp
from jax import lax
from jax.experimental import pallas as pl
from jax.experimental.pallas import tpu as pltpu
from jax.sharding import PartitionSpec as P

HDIM = 64
WIN = 64
QB = 64
KSEL = 64


NORM_EPS = 1e-05
MASKED = -1000000000.0


def from_behind(value, axis, steps):
    count = lax.axis_size(axis)
    first, last = (max(0, -steps), min(count, count - steps))
    return lax.ppermute(value, axis, [(source, source + steps) for source in range(first, last)])


def layer_norm(values, gain, shift):
    average = jnp.mean(values, axis=-1, keepdims=True)
    centred = values - average
    variance = jnp.mean(centred * centred, axis=-1, keepdims=True)
    return centred * lax.rsqrt(variance + NORM_EPS) * gain + shift


def gelu_tanh(values):
    return (
        0.5
        * values
        * (1.0 + jnp.tanh(0.7978845608028654 * (values + 0.044715 * values * values * values)))
    )


def gather_rows(row_block):
    return lax.all_gather(row_block, "tensor", axis=0, tiled=True)


def scatter_product(left_rows, weight, formula):
    return lax.psum_scatter(
        jnp.einsum(formula, left_rows, weight, preferred_element_type=jnp.float32).astype(
            jnp.bfloat16
        ),
        "tensor",
        scatter_dimension=0,
        tiled=True,
    ).astype(jnp.float32)


def near_slabs(full_rows, seq_start, seq_first, length_local):
    buckets = full_rows.shape[1]
    heads_local = full_rows.shape[2] // HDIM
    blocks = length_local // QB
    earlier = lax.dynamic_slice_in_dim(full_rows, jnp.maximum(seq_start - WIN, 0), WIN, 0)
    earlier = jnp.where(seq_first, jnp.zeros_like(earlier), earlier)
    local_part = lax.dynamic_slice_in_dim(full_rows, seq_start, length_local, 0)
    segment = jnp.concatenate([earlier, local_part], 0).reshape(
        length_local + WIN, buckets, heads_local, HDIM
    )
    return jnp.concatenate(
        [
            segment[offset_index * QB : offset_index * QB + length_local].reshape(
                blocks, QB, buckets, heads_local, HDIM
            )
            for offset_index in range(WIN // QB + 1)
        ],
        1,
    )


def far_rows(full_rows, flat_index):
    total_rows, buckets, feature_width = full_rows.shape
    heads_local = feature_width // HDIM
    return jnp.take(full_rows.reshape(total_rows * buckets * heads_local, HDIM), flat_index, axis=0)


def key_geometry(chosen_now, seq_start, blocks):
    buckets, heads_local = (chosen_now.shape[0], chosen_now.shape[1])
    bucket_ids = lax.broadcasted_iota(jnp.int32, chosen_now.shape, 0)
    head_ids = lax.broadcasted_iota(jnp.int32, chosen_now.shape, 1)
    flat_index = (chosen_now * buckets + bucket_ids) * heads_local + head_ids
    block_start = seq_start + QB * lax.broadcasted_iota(jnp.int32, (blocks, 1, 1), 0)
    query_ids = lax.broadcasted_iota(jnp.int32, (1, QB, 1), 1)
    key_ids = lax.broadcasted_iota(jnp.int32, (1, 1, WIN + QB), 2)
    distance = query_ids + WIN - key_ids
    near_ok = (distance >= 0) & (distance < WIN) & (block_start + key_ids - WIN >= 0)
    far_ok = chosen_now + WIN <= block_start.reshape(1, 1, blocks, 1)
    near_mask = jnp.broadcast_to(
        near_ok[:, None, None], (blocks, buckets, heads_local, QB, WIN + QB)
    )
    far_mask = jnp.broadcast_to(
        jnp.transpose(far_ok, (2, 0, 1, 3))[:, :, :, None, :],
        (blocks, buckets, heads_local, QB, KSEL),
    )
    return (flat_index, jnp.concatenate([near_mask, far_mask], -1))


def attention_setup(queries, key_rows, value_rows, chosen_now, seq_start, seq_first):
    length_local, buckets, feature_width = queries.shape
    heads_local = feature_width // HDIM
    blocks = length_local // QB
    query_blocks = queries.reshape(blocks, QB, buckets, heads_local, HDIM)
    flat_index, key_mask = key_geometry(chosen_now, seq_start, blocks)
    near_keys = near_slabs(key_rows, seq_start, seq_first, length_local)
    near_values = near_slabs(value_rows, seq_start, seq_first, length_local)
    far_keys = far_rows(key_rows, flat_index)
    far_values = far_rows(value_rows, flat_index)
    near_scores = jnp.einsum(
        "bqnhe,btnhe->bnhqt", query_blocks, near_keys, preferred_element_type=jnp.float32
    )
    far_scores = jnp.einsum(
        "bqnhe,nhbke->bnhqk", query_blocks, far_keys, preferred_element_type=jnp.float32
    )
    scores = jnp.where(
        key_mask, HDIM ** (-0.5) * jnp.concatenate([near_scores, far_scores], -1), MASKED
    )
    return (query_blocks, near_keys, near_values, far_keys, far_values, flat_index, scores)


def attend(queries, key_rows, value_rows, chosen_now, seq_start, seq_first):
    query_blocks, near_keys, near_values, far_keys, far_values, flat_index, scores = (
        attention_setup(queries, key_rows, value_rows, chosen_now, seq_start, seq_first)
    )
    span = WIN + QB
    row_top = jnp.max(scores, -1, keepdims=True)
    exp_terms = jnp.exp(scores - row_top)
    row_total = jnp.sum(exp_terms, -1, keepdims=True)
    softmax_low = (exp_terms / row_total).astype(jnp.bfloat16)
    near_part = jnp.einsum(
        "bnhqt,btnhe->bqnhe",
        softmax_low[..., :span],
        near_values,
        preferred_element_type=jnp.float32,
    )
    far_part = jnp.einsum(
        "bnhqk,nhbke->bqnhe",
        softmax_low[..., span:],
        far_values,
        preferred_element_type=jnp.float32,
    )
    return ((near_part + far_part).reshape(queries.shape), row_top + jnp.log(row_total))


def spread_back(near_grad, far_grad, flat_index, seq_start, seq_first, total_rows):
    blocks, span, buckets, heads_local, head_size = near_grad.shape
    length_local = blocks * QB
    feature_width = heads_local * head_size
    segment = jnp.zeros((length_local + WIN, buckets, heads_local, head_size), jnp.float32)
    for offset_index in range(WIN // QB + 1):
        piece = near_grad[:, offset_index * QB : (offset_index + 1) * QB].reshape(
            length_local, buckets, heads_local, head_size
        )
        segment = segment.at[offset_index * QB : offset_index * QB + length_local].add(piece)
    full_rows = jnp.zeros((total_rows * buckets * heads_local, head_size), jnp.float32)
    full_rows = full_rows.at[flat_index.reshape(-1)].add(far_grad.reshape(-1, head_size))
    full_rows = full_rows.reshape(total_rows, buckets, feature_width)
    local_part = segment[WIN:].reshape(length_local, buckets, feature_width)
    earlier = jnp.where(seq_first, 0.0, segment[:WIN].reshape(WIN, buckets, feature_width))
    full_rows = lax.dynamic_update_slice_in_dim(
        full_rows,
        lax.dynamic_slice_in_dim(full_rows, seq_start, length_local, 0) + local_part,
        seq_start,
        0,
    )
    earlier_start = jnp.maximum(seq_start - WIN, 0)
    full_rows = lax.dynamic_update_slice_in_dim(
        full_rows,
        lax.dynamic_slice_in_dim(full_rows, earlier_start, WIN, 0) + earlier,
        earlier_start,
        0,
    )
    return full_rows


def attend_back(
    queries, key_rows, value_rows, chosen_now, seq_start, seq_first, log_total, grad_mixed
):
    query_blocks, near_keys, near_values, far_keys, far_values, flat_index, scores = (
        attention_setup(queries, key_rows, value_rows, chosen_now, seq_start, seq_first)
    )
    span = WIN + QB
    score_scale = HDIM ** (-0.5)
    grad_blocks = grad_mixed.reshape(query_blocks.shape)
    weights_full = jnp.exp(scores - log_total)
    softmax_low = weights_full.astype(jnp.bfloat16)
    grad_near_weights = jnp.einsum(
        "bqnhe,btnhe->bnhqt", grad_blocks, near_values, preferred_element_type=jnp.float32
    )
    grad_far_weights = jnp.einsum(
        "bqnhe,nhbke->bnhqk", grad_blocks, far_values, preferred_element_type=jnp.float32
    )
    grad_weights = jnp.concatenate([grad_near_weights, grad_far_weights], -1)
    row_dot = jnp.sum(weights_full * grad_weights, -1, keepdims=True)
    grad_scores = (weights_full * (grad_weights - row_dot)).astype(jnp.bfloat16)
    grad_near, grad_far = (grad_scores[..., :span], grad_scores[..., span:])
    grad_queries = score_scale * (
        jnp.einsum("bnhqt,btnhe->bqnhe", grad_near, near_keys, preferred_element_type=jnp.float32)
        + jnp.einsum("bnhqk,nhbke->bqnhe", grad_far, far_keys, preferred_element_type=jnp.float32)
    )
    near_key_grad = score_scale * jnp.einsum(
        "bnhqt,bqnhe->btnhe", grad_near, query_blocks, preferred_element_type=jnp.float32
    )
    far_key_grad = score_scale * jnp.einsum(
        "bnhqk,bqnhe->nhbke", grad_far, query_blocks, preferred_element_type=jnp.float32
    )
    near_value_grad = jnp.einsum(
        "bnhqt,bqnhe->btnhe",
        softmax_low[..., :span],
        grad_blocks,
        preferred_element_type=jnp.float32,
    )
    far_value_grad = jnp.einsum(
        "bnhqk,bqnhe->nhbke",
        softmax_low[..., span:],
        grad_blocks,
        preferred_element_type=jnp.float32,
    )
    total_rows = key_rows.shape[0]
    key_grad = spread_back(
        near_key_grad, far_key_grad, flat_index, seq_start, seq_first, total_rows
    )
    value_grad = spread_back(
        near_value_grad, far_value_grad, flat_index, seq_start, seq_first, total_rows
    )
    return (grad_queries.reshape(queries.shape), key_grad, value_grad)


def forward_pass(hidden, params, chosen_now, query_mask, seq_start, seq_first, finish):
    (
        ln1_gain,
        ln1_shift,
        w_qkv,
        b_qv,
        w_out,
        b_out,
        ln2_gain,
        ln2_shift,
        w_fc,
        b_fc,
        w_proj,
        b_proj,
    ) = params
    hidden_wide = hidden.astype(jnp.float32)
    normed_all = gather_rows(layer_norm(hidden_wide, ln1_gain, ln1_shift).astype(jnp.bfloat16))
    projected = jnp.einsum("pnd,jdc->jpnc", normed_all, w_qkv, preferred_element_type=jnp.float32)
    queries = (projected[0] + b_qv[0]).astype(jnp.bfloat16)
    key_rows, value_rows = (
        lax.all_gather(projected[1].astype(jnp.bfloat16), "seq", axis=0, tiled=True),
        lax.all_gather((projected[2] + b_qv[1]).astype(jnp.bfloat16), "seq", axis=0, tiled=True),
    )
    attended, log_total = attend(queries, key_rows, value_rows, chosen_now, seq_start, seq_first)
    mixed_rows = (attended * query_mask[:, :, None]).astype(jnp.bfloat16)
    middle = hidden_wide + scatter_product(mixed_rows, w_out, "pnc,cd->pnd") + b_out
    normed_mlp = gather_rows(layer_norm(middle, ln2_gain, ln2_shift).astype(jnp.bfloat16))
    pre_active = (
        jnp.einsum("pnd,df->pnf", normed_mlp, w_fc, preferred_element_type=jnp.float32) + b_fc
    )
    active = gelu_tanh(pre_active).astype(jnp.bfloat16)
    if not finish:
        return (
            normed_all,
            queries,
            key_rows,
            value_rows,
            log_total,
            mixed_rows,
            middle,
            normed_mlp,
            pre_active,
            active,
        )
    output = (middle + scatter_product(active, w_proj, "pnf,fd->pnd") + b_proj).astype(jnp.bfloat16)
    return (output, (key_rows, value_rows))


def backward_pass(hidden, upstream, params, chosen_now, query_mask, seq_start, seq_first):
    (
        ln1_gain,
        ln1_shift,
        w_qkv,
        b_qv,
        w_out,
        b_out,
        ln2_gain,
        ln2_shift,
        w_fc,
        b_fc,
        w_proj,
        b_proj,
    ) = params
    (
        normed_all,
        queries,
        key_rows,
        value_rows,
        log_total,
        mixed_rows,
        middle,
        normed_mlp,
        pre_active,
        active,
    ) = forward_pass(hidden, params, chosen_now, query_mask, seq_start, seq_first, False)
    upstream_all = gather_rows(upstream)
    grad_w_proj = jnp.einsum(
        "pnf,pnd->fd", active, upstream_all, preferred_element_type=jnp.float32
    )
    grad_b_proj = jnp.sum(upstream.astype(jnp.float32), axis=(0, 1))
    grad_active = jnp.einsum(
        "pnd,fd->pnf", upstream_all, w_proj, preferred_element_type=jnp.float32
    )
    unused_value, gelu_pull = jax.vjp(gelu_tanh, pre_active)
    grad_pre = gelu_pull(grad_active)[0].astype(jnp.bfloat16)
    grad_w_fc = jnp.einsum("pnd,pnf->df", normed_mlp, grad_pre, preferred_element_type=jnp.float32)
    grad_b_fc = jnp.sum(grad_pre.astype(jnp.float32), axis=(0, 1))
    grad_normed_mlp = scatter_product(grad_pre, w_fc, "pnf,df->pnd")
    unused_norm, second_pull = jax.vjp(layer_norm, middle, ln2_gain, ln2_shift)
    grad_mid_norm, grad_ln2_gain, grad_ln2_shift = second_pull(grad_normed_mlp)
    grad_middle = upstream.astype(jnp.float32) + grad_mid_norm
    grad_branch = grad_middle.astype(jnp.bfloat16)
    grad_b_out = jnp.sum(grad_branch.astype(jnp.float32), axis=(0, 1))
    branch_all = gather_rows(grad_branch)
    grad_w_out = jnp.einsum(
        "pnc,pnd->cd", mixed_rows, branch_all, preferred_element_type=jnp.float32
    )
    grad_mixed = jnp.einsum(
        "pnd,cd->pnc", branch_all, w_out, preferred_element_type=jnp.float32
    ).astype(jnp.bfloat16) * query_mask[:, :, None].astype(jnp.bfloat16)
    grad_queries, key_grad_all, value_grad_all = attend_back(
        queries, key_rows, value_rows, chosen_now, seq_start, seq_first, log_total, grad_mixed
    )
    key_grad, value_grad = (
        lax.psum_scatter(
            key_grad_all.astype(jnp.bfloat16), "seq", scatter_dimension=0, tiled=True
        ).astype(jnp.float32),
        lax.psum_scatter(
            value_grad_all.astype(jnp.bfloat16), "seq", scatter_dimension=0, tiled=True
        ).astype(jnp.float32),
    )
    grad_project = jnp.stack(
        [
            grad_queries.astype(jnp.bfloat16),
            key_grad.astype(jnp.bfloat16),
            value_grad.astype(jnp.bfloat16),
        ],
        2,
    )
    grad_w_qkv = jnp.einsum(
        "pnd,pnjc->jdc", normed_all, grad_project, preferred_element_type=jnp.float32
    )
    grad_b_qv = jnp.sum(grad_project[:, :, 0::2].astype(jnp.float32), axis=(0, 1))
    grad_normed = scatter_product(grad_project, w_qkv, "pnjc,jdc->pnd")
    unused_first, first_pull = jax.vjp(layer_norm, hidden.astype(jnp.float32), ln1_gain, ln1_shift)
    grad_in_norm, grad_ln1_gain, grad_ln1_shift = first_pull(grad_normed)
    grad_hidden = (grad_middle + grad_in_norm).astype(jnp.bfloat16)
    block_grads = (
        grad_ln1_gain,
        grad_ln1_shift,
        grad_w_qkv,
        grad_b_qv,
        grad_w_out,
        grad_b_out,
        grad_ln2_gain,
        grad_ln2_shift,
        grad_w_fc,
        grad_b_fc,
        grad_w_proj,
        grad_b_proj,
    )
    return (grad_hidden, block_grads)


def on_device(
    inputs,
    cotangent,
    lengths,
    chosen,
    ln1_gain,
    ln1_shift,
    w_qkv,
    b_qv,
    w_out,
    b_out,
    ln2_gain,
    ln2_shift,
    w_fc,
    b_fc,
    w_proj,
    b_proj,
):
    params = tuple(
        (
            weight_array[0]
            for weight_array in (
                ln1_gain,
                ln1_shift,
                w_qkv,
                b_qv,
                w_out,
                b_out,
                ln2_gain,
                ln2_shift,
                w_fc,
                b_fc,
                w_proj,
                b_proj,
            )
        )
    )
    section_index = lax.axis_index("section")
    section_count = lax.axis_size("section")
    seq_index = lax.axis_index("seq")
    tensor_index = lax.axis_index("tensor")
    tensor_count = lax.axis_size("tensor")
    micro_count, rows_local, buckets, feature_width = inputs.shape
    length_local = rows_local * tensor_count
    heads_width = w_qkv.shape[-1]
    seq_start = seq_index * length_local
    seq_first = seq_index == 0
    positions = seq_start + lax.broadcasted_iota(jnp.int32, (micro_count, length_local, buckets), 1)
    mask_all = (positions < lengths[:, None, :]).astype(jnp.float32)
    mask_rows = lax.dynamic_slice_in_dim(mask_all, tensor_index * rows_local, rows_local, 1)
    step_count = micro_count + section_count - 1
    chosen_section = chosen[0]
    received = jnp.zeros((rows_local, buckets, feature_width), jnp.bfloat16)
    stored = jnp.zeros((micro_count, rows_local, buckets, feature_width), jnp.bfloat16)
    outputs = jnp.zeros_like(stored)
    for step_index in range(step_count):
        micro_index = step_index - section_index
        running = (micro_index >= 0) & (micro_index < micro_count)
        slot_index = jnp.clip(micro_index, 0, micro_count - 1)
        block_in = jnp.where(
            section_index == 0, lax.dynamic_index_in_dim(inputs, slot_index, 0, False), received
        )
        chosen_now = lax.dynamic_index_in_dim(chosen_section, slot_index, 0, False)
        query_mask = lax.dynamic_index_in_dim(mask_all, slot_index, 0, False)
        result, key_pair = forward_pass(
            block_in, params, chosen_now, query_mask, seq_start, seq_first, True
        )
        stored = jnp.where(
            running, lax.dynamic_update_index_in_dim(stored, block_in, slot_index, 0), stored
        )
        outputs = jnp.where(
            running, lax.dynamic_update_index_in_dim(outputs, result, slot_index, 0), outputs
        )
        received = from_behind(result, "section", 1)
    back_received = jnp.zeros((rows_local, buckets, feature_width), jnp.bfloat16)
    in_grads = jnp.zeros_like(stored)
    totals = None
    for step_index in range(step_count):
        micro_index = step_index - (section_count - 1 - section_index)
        running = (micro_index >= 0) & (micro_index < micro_count)
        slot_index = jnp.clip(micro_index, 0, micro_count - 1)
        chosen_now = lax.dynamic_index_in_dim(chosen_section, slot_index, 0, False)
        query_mask = lax.dynamic_index_in_dim(mask_all, slot_index, 0, False)
        local_mask = lax.dynamic_index_in_dim(mask_rows, slot_index, 0, False)
        top_grad = (
            lax.dynamic_index_in_dim(cotangent, slot_index, 0, False).astype(jnp.float32)
            * local_mask[:, :, None]
        ).astype(jnp.bfloat16)
        upstream = jnp.where(section_index == section_count - 1, top_grad, back_received)
        hidden = lax.dynamic_index_in_dim(stored, slot_index, 0, False)
        grad_hidden, block_grads = backward_pass(
            hidden, upstream, params, chosen_now, query_mask, seq_start, seq_first
        )
        block_grads = tuple(
            (jnp.where(running, grad_part, jnp.zeros_like(grad_part)) for grad_part in block_grads)
        )
        totals = (
            block_grads
            if step_index == 0
            else tuple(
                (total_part + grad_part for total_part, grad_part in zip(totals, block_grads))
            )
        )
        in_grads = jnp.where(
            running, lax.dynamic_update_index_in_dim(in_grads, grad_hidden, slot_index, 0), in_grads
        )
        back_received = from_behind(grad_hidden, "section", -1)
    (
        sum_ln1_gain,
        sum_ln1_shift,
        sum_w_qkv,
        sum_b_qv,
        sum_w_out,
        sum_b_out,
        sum_ln2_gain,
        sum_ln2_shift,
        sum_w_fc,
        sum_b_fc,
        sum_w_proj,
        sum_b_proj,
    ) = totals
    part_qkv, part_out, part_fc, part_proj = (
        lax.psum_scatter(
            sum_w_qkv.astype(jnp.bfloat16), "seq", scatter_dimension=1, tiled=True
        ).astype(jnp.float32),
        lax.psum_scatter(
            sum_w_out.astype(jnp.bfloat16), "seq", scatter_dimension=1, tiled=True
        ).astype(jnp.float32),
        lax.psum_scatter(
            sum_w_fc.astype(jnp.bfloat16), "seq", scatter_dimension=0, tiled=True
        ).astype(jnp.float32),
        lax.psum_scatter(
            sum_w_proj.astype(jnp.bfloat16), "seq", scatter_dimension=1, tiled=True
        ).astype(jnp.float32),
    )
    bias_qv = lax.dynamic_update_slice_in_dim(
        jnp.zeros((2, feature_width), jnp.float32), sum_b_qv, tensor_index * heads_width, 1
    )
    units_local = sum_b_fc.shape[0]
    bias_fc = lax.dynamic_update_slice_in_dim(
        jnp.zeros((units_local * tensor_count,), jnp.float32),
        sum_b_fc,
        tensor_index * units_local,
        0,
    )
    small_sums = lax.psum(
        (
            sum_ln1_gain,
            sum_ln1_shift,
            bias_qv,
            sum_b_out,
            sum_ln2_gain,
            sum_ln2_shift,
            bias_fc,
            sum_b_proj,
        ),
        ("seq", "tensor"),
    )
    return (
        outputs[None],
        in_grads[None],
        small_sums[0][None],
        small_sums[1][None],
        part_qkv[None],
        small_sums[2][None],
        part_out[None],
        small_sums[3][None],
        small_sums[4][None],
        small_sums[5][None],
        part_fc[None],
        small_sums[6][None],
        part_proj[None],
        small_sums[7][None],
    )


STREAMS = 4
NRM, NMLP, UPS, BRN, ACT, GPRE, MIX, DQKV = range(8)
F32 = jnp.float32
LOW = jnp.bfloat16
MESH_ID = pl.DeviceIdType.MESH


def dot_nn(left, right):
    return lax.dot_general(left, right, (((1,), (0,)), ((), ())), preferred_element_type=F32)


def dot_nt(left, right):
    return lax.dot_general(left, right, (((1,), (1,)), ((), ())), preferred_element_type=F32)


def dot_tn(left, right):
    return lax.dot_general(left, right, (((0,), (0,)), ((), ())), preferred_element_type=F32)


def standard(rows):
    centred = rows - jnp.mean(rows, axis=-1, keepdims=True)
    scale = lax.rsqrt(jnp.mean(centred * centred, axis=-1, keepdims=True) + NORM_EPS)
    return centred * scale, scale


def standard_back(grad, xhat, scale):
    inner = jnp.mean(grad * xhat, axis=-1, keepdims=True)
    return scale * (grad - jnp.mean(grad, axis=-1, keepdims=True) - xhat * inner)


def column_sum(rows):
    return jnp.sum(rows.astype(F32), axis=0, keepdims=True)


def relay_kernel(names, *refs):
    r = types.SimpleNamespace(**dict(zip(names, refs)))
    a, c, t = (lax.axis_index(name) for name in ("section", "seq", "tensor"))
    lines = lax.axis_size("section")
    chips = lax.axis_size("tensor")
    rows, buckets, width = r.inputs.shape[1:]
    half_width = width // 2
    local = rows * chips
    total = 2 * local
    stream_rows = local // STREAMS
    head_width = r.wo_in.shape[0]
    heads = head_width // HDIM
    blocks = local // QB
    units = r.wp_in.shape[0]
    scale = HDIM ** (-0.5)
    streams = range(STREAMS)

    def remote(src, dst, send, recv, **target):
        return pltpu.make_async_remote_copy(
            src_ref=src,
            dst_ref=dst,
            send_sem=send,
            recv_sem=recv,
            device_id=target,
            device_id_type=MESH_ID,
        )

    def drain(ref, sem):
        pltpu.make_async_copy(ref, ref, sem).wait()

    def row_block(index, size):
        return pl.ds(pl.multiple_of(index * size, size), size)

    near_chip = t + 1 - 2 * (t % 2)
    over_chip = (t + 2) % 4
    across_chip = 3 - t
    middle_chip = (t == 1) | (t == 2)
    end_chip = (t == 0) | (t == 3)
    owned = stream_rows // 2
    mine = row_block(t - 1, owned)
    my_half = row_block(c, local)

    barrier = pltpu.get_barrier_semaphore()
    for core in range(2):
        for step in range(1, chips):
            there = {"tensor": (t + step) % chips, "seq": core}
            pl.semaphore_signal(barrier, inc=1, device_id=there, device_id_type=MESH_ID)
        for step in range(1, lines):
            there = {"section": (a + step) % lines, "seq": core}
            pl.semaphore_signal(barrier, inc=1, device_id=there, device_id_type=MESH_ID)
    for step in range(1, lines):
        there = {"section": (a + step) % lines, "tensor": near_chip}
        pl.semaphore_signal(barrier, inc=1, device_id=there, device_id_type=MESH_ID)
    pl.semaphore_signal(barrier, inc=1, device_id={"seq": 1 - c}, device_id_type=MESH_ID)
    pl.semaphore_wait(barrier, 2 * (chips - 1) + 3 * (lines - 1) + 1)

    def beside(s):
        return s + 1 - 2 * (s % 2)

    def above(s):
        return (s + 2) % 4

    def store(p):
        return (r.wq, r.wo, r.wf, r.wp)[p]

    def source(p):
        return (r.wq_in, r.wo_in, r.wf_in, r.wp_in)[p]

    def height(p):
        return source(p).shape[0]

    def core_half(p, s, core):
        return store(p).at[s, row_block(core, height(p) // 2)]

    def first_hop(p, s, neighbour, which):
        return remote(
            source(p).at[row_block(c, height(p) // 2)],
            core_half(p, s, c),
            r.w_first_s.at[p, which],
            r.w_first_r.at[s, p],
            section=neighbour,
        )

    def second_hop(p, s, which):
        view = store(p).at[s, row_block(2 * c + which, height(p) // 4)]
        return remote(
            view, view, r.w_second_s.at[s, p], r.w_second_r.at[s, p, which], section=3 - s
        )

    def core_hop(p, s, core):
        view = core_half(p, s, core)
        return remote(view, view, r.w_core_s.at[s, p], r.w_core_r.at[s, p], seq=1 - c)

    def own_copy(p):
        return pltpu.make_async_copy(source(p), store(p).at[a], r.w_own.at[p])

    def pass_on(s, p, which):
        line = (beside(s), above(s))[which]

        @pl.when(a == line)
        def _():
            first_hop(p, s, line, which).wait_recv()
            second_hop(p, s, which).start()
            core_hop(p, s, c).start()

    def pass_all(s, pieces):
        for p in pieces:
            for which in range(2):
                pass_on(s, p, which)

    def pass_far(s, p):
        @pl.when(a == 3 - s)
        def _():
            second_hop(p, s, 0).wait_recv()
            second_hop(p, s, 1).wait_recv()
            core_hop(p, s, c).start()

    def need(s, p):
        @pl.when(s == 0)
        def _():
            if p < 2:
                pass_all(0, (p,))
            pass_far(0, p)

        @pl.when(a == s)
        def _():
            own_copy(p).wait()

        @pl.when(a != s)
        def _():
            core_hop(p, s, 1 - c).wait_recv()

    def small_copy(step, line, slot):
        return remote(
            r.small_own, r.small.at[slot], r.small_s.at[step], r.small_r.at[slot], section=line
        )

    def count_copy(step, line, slot):
        return remote(
            r.count_own.at[line],
            r.count.at[slot],
            r.count_s.at[step],
            r.count_r.at[slot],
            section=line,
        )

    singles = (r.ln1_gain, r.ln1_shift, r.ln2_gain, r.ln2_shift, r.b_out, r.b_proj)
    for place, single in enumerate(singles):
        r.small_own[place : place + 1] = single[...]
    r.small_own[6:7, :units] = r.b_fc[...]
    r.small_own[7:8, :head_width] = r.b_qv[0:1]
    r.small_own[7:8, half_width : half_width + head_width] = r.b_qv[1:2]
    for step in range(1, lines):
        small_copy(step - 1, (a + step) % lines, a).start()
    for p in range(4):
        for which, line in enumerate((beside(a), above(a))):
            first_hop(p, a, line, which).start()
    for p in range(4):
        own_copy(p).start()
    r.small[a] = r.small_own[...]

    def place_of(index):
        inside = index % local
        stream, left = inside // stream_rows, inside % stream_rows
        first = (index // local) * local + (left // owned) * (local // 2)
        return first + stream * owned + left % owned

    def iota(shape, dimension):
        return lax.broadcasted_iota(jnp.int32, shape, dimension)

    square = jnp.where(iota((KSEL, KSEL), 0) == iota((KSEL, KSEL), 1), 1.0, 0.0).astype(LOW)
    position = place_of(iota((KSEL, total), 1)).astype(F32)
    for pair in range(lines * heads):
        line, head = pair // heads, pair % heads
        columns = dot_nt(square, r.chosen[pair].astype(F32).astype(LOW))
        for block in range(blocks):
            pick = head * blocks + block
            r.count_own[line, pick : pick + 1, :] = jnp.sum(
                jnp.where(columns[:, block : block + 1] == position, 1.0, 0.0),
                axis=0,
                keepdims=True,
            )
    for step in range(1, lines):
        count_copy(step - 1, (a + step) % lines, a).start()
    r.count[a] = r.count_own[a]

    NEAR, OVER, ACROSS = range(3)

    def gather(buffer, s, kind, j, owner, target, slot):
        view = buffer.at[s, j, row_block(owner - 1, owned)]
        return remote(
            view, view, r.ag_s.at[kind, j, slot], r.ag_r.at[kind, j, slot], tensor=target
        )

    def gather_start(buffer, s, kind, j):
        gather(buffer, s, kind, j, t, over_chip, OVER).start()
        gather(buffer, s, kind, j, t, across_chip, ACROSS).start()
        gather(buffer, s, kind, j, t, near_chip, NEAR).start()

    def gather_wait(buffer, s, kind, j):
        @pl.when(middle_chip)
        def _():
            gather(buffer, s, kind, j, across_chip, across_chip, ACROSS).wait_recv()

        @pl.when(end_chip)
        def _():
            gather(buffer, s, kind, j, near_chip, near_chip, NEAR).wait_recv()
            gather(buffer, s, kind, j, over_chip, over_chip, OVER).wait_recv()

    def gather_sent(buffer, s, kind, j):
        @pl.when(middle_chip)
        def _():
            gather(buffer, s, kind, j, t, over_chip, OVER).wait_send()
            gather(buffer, s, kind, j, t, across_chip, ACROSS).wait_send()
            gather(buffer, s, kind, j, t, near_chip, NEAR).wait_send()

    def scatter(s, kind, j, owner, slot):
        return remote(
            r.part.at[kind, j, row_block(owner - 1, owned)],
            r.arrived.at[s, kind, j, slot],
            r.rs_s.at[kind, j, slot],
            r.rs_r.at[kind, j, slot],
            tensor=owner,
        )

    def scatter_start(s, kind, j, product):
        r.part[kind, j] = product.astype(LOW)

        @pl.when(end_chip)
        def _():
            scatter(s, kind, j, over_chip, OVER).start()
            scatter(s, kind, j, near_chip, NEAR).start()

        @pl.when(middle_chip)
        def _():
            scatter(s, kind, j, across_chip, ACROSS).start()

    def scatter_sum(s, kind, j):
        result = r.part[kind, j, mine].astype(F32)
        for slot in (NEAR, ACROSS, OVER):
            scatter(s, kind, j, t, slot).wait_recv()
            result = result + r.arrived[s, kind, j, slot].astype(F32)
        return result

    def scatter_sent(s, kind, j):
        @pl.when(end_chip)
        def _():
            scatter(s, kind, j, over_chip, OVER).wait_send()
            scatter(s, kind, j, near_chip, NEAR).wait_send()

        @pl.when(middle_chip)
        def _():
            scatter(s, kind, j, across_chip, ACROSS).wait_send()

    own_rows = (r.nrm, r.nmlp, r.ups, r.brn, r.act, r.gpre, r.mix, r.dqkv)
    all_rows = (
        r.all_nrm,
        r.all_nmlp,
        r.all_ups,
        r.all_brn,
        r.all_act,
        r.all_gpre,
        r.all_mix,
        r.all_dqkv,
    )

    def rows_copy(index, s, same, stays=False):
        core = c if same else 1 - c
        src = own_rows[index].at[s]
        dst = all_rows[index].at[a, c]
        if index <= BRN:
            src = src.at[:, :, row_block(core, half_width)]
        recv = r.rows_r.at[index]
        if stays:
            return pltpu.make_async_copy(src, dst, recv)
        if same:
            return remote(src, dst, r.rows_s.at[index, s, 0], recv, section=s)
        return remote(src, dst, r.rows_s.at[index, s, 1], recv, section=s, seq=1 - c)

    def rows_start(index, s):
        @pl.when(a == s)
        def _():
            rows_copy(index, s, True, True).start()

        @pl.when(a != s)
        def _():
            rows_copy(index, s, True).start()

        if index <= BRN:
            rows_copy(index, s, False).start()

    def forward_rows(s):
        for index in (NRM, MIX, NMLP, ACT):
            rows_start(index, s)

    def rows_sent(index, s):
        @pl.when(a != s)
        def _():
            rows_copy(index, s, True).wait_send()

        if index <= BRN:
            rows_copy(index, s, False).wait_send()

    def share_copy(index, core):
        view = all_rows[index].at[:, core]
        return remote(view, view, r.share_s.at[index - ACT], r.share_r.at[index - ACT], seq=1 - c)

    def share(index):
        drain(all_rows[index].at[:, c], r.rows_r.at[index])
        share_copy(index, c).start()

    def norm_copy(s):
        return remote(
            r.norm_part.at[s], r.norm_all.at[a], r.norm_s.at[s], r.norm_r, section=s
        )

    def norm_start(s):
        @pl.when(a == s)
        def _():
            pltpu.make_async_copy(r.norm_part.at[s], r.norm_all.at[a], r.norm_r).start()

        @pl.when(a != s)
        def _():
            norm_copy(s).start()

    def home_copy(what, s, chip):
        src, dst, send, recv = what
        return remote(
            src.at[s, chip % 2],
            dst.at[a],
            send.at[s, chip % 2],
            recv,
            section=s,
            tensor=chip,
        )

    def home_start(what, s):
        src, dst, send, recv = what

        @pl.when(middle_chip & (a == s))
        def _():
            pltpu.make_async_copy(src.at[s, t % 2], dst.at[a], recv).start()

        @pl.when(middle_chip & (a != s))
        def _():
            home_copy(what, s, t).start()

        @pl.when(middle_chip)
        def _():
            home_copy(what, s, near_chip).start()

    def home_sent(what, s):
        @pl.when(middle_chip & (a != s))
        def _():
            home_copy(what, s, t).wait_send()

        @pl.when(middle_chip)
        def _():
            home_copy(what, s, near_chip).wait_send()

    out_home = (r.out_low, r.acts, r.out_s, r.out_r)
    grad_home = (r.grad_low, r.grads, r.grad_s, r.grad_r)

    length = r.lengths[a // buckets, a % buckets]
    key = place_of(iota((stream_rows, total), 1))
    for j in streams:
        query = place_of(c * local + j * stream_rows + iota((stream_rows, total), 0))
        r.near[j] = jnp.where((query >= key) & (query - key < WIN), 1.0, 0.0)
    key_row = place_of(iota((1, total), 1))

    def row_mask(place):
        return jnp.where(place < length, 1.0, 0.0)

    def multiplicity(s, j, head):
        far = []
        for block in range(blocks):
            pick = head * blocks + block
            limit = (c * blocks + block) * QB - WIN
            counted = jnp.where(key_row <= limit, r.count[s, pick : pick + 1, :], 0.0)
            far.append(jnp.broadcast_to(counted, (stream_rows // blocks, total)))
        return r.near[j] + jnp.concatenate(far, axis=0)

    def head_cols(head):
        return slice(head * HDIM, (head + 1) * HDIM)

    def kv_copy(s):
        view = r.kv.at[s, :, 0:local]
        return remote(view, view, r.kv_s.at[s], r.kv_r.at[s], seq=1 - c)

    def dkv_copy(s):
        return remote(r.dkv_out.at[s], r.dkv_in.at[s], r.dkv_s.at[s], r.dkv_r.at[s], seq=1 - c)

    def own_sequence(ref):
        both = ref[a // buckets].astype(F32)
        picked = both[:, 0, :]
        for bucket in range(1, buckets):
            picked = jnp.where(a % buckets == bucket, both[:, bucket, :], picked)
        return picked

    def own_part(j):
        chip, first = (j * owned) // rows, (j * owned) % rows
        return chip, slice(first, first + owned)

    def first_copy():
        return remote(r.first_out, r.first_in, r.first_s, r.first_r, tensor=near_chip)

    own_place = c * local + t * rows + iota((rows, 1), 0)
    r.first_out[0] = own_sequence(r.inputs).astype(LOW)
    r.first_out[1] = (own_sequence(r.cotangent) * row_mask(own_place)).astype(LOW)
    r.norm_part[...] = jnp.zeros_like(r.norm_part)

    @pl.when(c == 0)
    def _():
        r.kv[:, :, local:total] = jnp.zeros((lines, 2, local, head_width), LOW)


    @pl.when(end_chip)
    def _():
        first_copy().start()

    @pl.when(middle_chip)
    def _():
        first_copy().wait_recv()
        for which in range(2):
            here, beside_it = r.first_out[which].astype(F32), r.first_in[which].astype(F32)
            lower = jnp.where(t % 2 == 0, here, beside_it)
            upper = jnp.where(t % 2 == 0, beside_it, here)
            for j in streams:
                chip, part = own_part(j)
                own_block = (lower, upper)[chip][part]
                if which == 0:
                    r.hidden[j] = own_block
                else:
                    r.upstream[j] = own_block.astype(LOW)

    def on_owner(stage):
        def run(s, j):
            @pl.when(middle_chip)
            def _():
                stage(s, j)

        return run

    def keep_rows(target, s, j, result):
        chip, part = own_part(j)
        target[s, chip, part] = result

    @on_owner
    def enter(s, j):
        xhat, inverse = standard(r.hidden[j])
        r.xhat1[s, j] = xhat
        r.inv1[s, j] = jnp.broadcast_to(inverse, (owned, 128))
        r.nrm[s, j, mine] = (xhat * r.small[s, 0:1] + r.small[s, 1:2]).astype(LOW)
        gather_start(r.nrm, s, 0, j)

    def project(s, j):
        gather_wait(r.nrm, s, 0, j)
        normed = r.nrm[s, j]
        place = row_block(c * STREAMS + j, stream_rows)
        bias_v = r.small[s, 7:8, half_width : half_width + head_width]
        key_rows = dot_nt(normed, r.wq[s, head_width : 2 * head_width])
        value_rows = dot_nt(normed, r.wq[s, 2 * head_width : 3 * head_width]) + bias_v
        r.kv[s, 0, place] = key_rows.astype(LOW)
        r.kv[s, 1, place] = value_rows.astype(LOW)
        gather_sent(r.nrm, s, 0, j)

    def ask(s, j):
        queries = dot_nt(r.nrm[s, j], r.wq[s, 0:head_width]) + r.small[s, 7:8, :head_width]
        r.qry[s, j] = queries.astype(LOW)

    def attend_line(s, j):
        mixed = []
        for head in range(heads):
            cols = head_cols(head)
            times = multiplicity(s, j, head)
            scores = scale * dot_nt(r.qry[s, j, :, cols], r.kv[s, 0, :, cols])
            scores = jnp.where(times > 0.0, scores, MASKED)
            top = jnp.max(scores, axis=-1, keepdims=True)
            terms = times * jnp.exp(scores - top)
            weights = terms / jnp.sum(terms, axis=-1, keepdims=True)
            r.soft[s, j, head] = weights
            mixed.append(dot_nn(weights.astype(LOW), r.kv[s, 1, :, cols]))
        mask = row_mask(place_of(c * local + j * stream_rows + iota((stream_rows, 1), 0)))
        r.mix[s, j] = (jnp.concatenate(mixed, axis=-1) * mask).astype(LOW)

    def leave_attention(s, j):
        scatter_start(s, 0, j, dot_nn(r.mix[s, j], r.wo[s]))

    @on_owner
    def between(s, j):
        middle = r.hidden[j] + scatter_sum(s, 0, j) + r.small[s, 4:5]
        r.middle[j] = middle
        xhat, inverse = standard(middle)
        r.xhat2[s, j] = xhat
        r.inv2[s, j] = jnp.broadcast_to(inverse, (owned, 128))
        r.nmlp[s, j, mine] = (xhat * r.small[s, 2:3] + r.small[s, 3:4]).astype(LOW)
        gather_start(r.nmlp, s, 1, j)

    def feed(s, j):
        gather_wait(r.nmlp, s, 1, j)
        before = dot_nn(r.nmlp[s, j], r.wf[s]) + r.small[s, 6:7, :units]
        bend = jnp.tanh(0.7978845608028654 * (before + 0.044715 * before * before * before))
        r.act[s, j] = (0.5 * before * (1.0 + bend)).astype(LOW)
        r.slope[s, j] = 0.5 * (1.0 + bend) + 0.5 * before * (1.0 - bend * bend) * (
            0.7978845608028654 * (1.0 + 3 * 0.044715 * before * before)
        )

        gather_sent(r.nmlp, s, 1, j)

    def leave_feed(s, j):
        scatter_start(s, 1, j, dot_nn(r.act[s, j], r.wp[s]))

    @on_owner
    def finish(s, j):
        result = r.middle[j] + scatter_sum(s, 1, j) + r.small[s, 5:6]
        keep_rows(r.out_low, s, j, result.astype(LOW))
        r.hidden[j] = result.astype(LOW).astype(F32)

    def small_ready(s):
        @pl.when(a != s)
        def _():
            small_copy(0, a, s).wait_recv()

    small_ready(0)
    for j in streams:
        enter(0, j)

    def forward(s, _):
        need(s, 0)
        for j in streams:
            project(s, j)

        @pl.when(c == 0)
        def _():
            kv_copy(s).start()

        for j in streams:
            ask(s, j)

        @pl.when(a != s)
        def _():
            count_copy(0, a, s).wait_recv()

        @pl.when(c == 1)
        def _():
            kv_copy(s).wait_recv()

        for j in streams:
            attend_line(s, j)
            if j == 0:
                need(s, 1)
            leave_attention(s, j)

        @pl.when(s == 0)
        def _():
            pass_all(0, (2,))
            for later in range(1, lines):
                pass_all(later, (0, 1, 2))

        @pl.when(s == 1)
        def _():
            pass_far(1, 2)
            pass_far(1, 3)
            for later in range(2, lines):
                for p in range(4):
                    pass_far(later, p)

        for j in streams:
            between(s, j)
            scatter_sent(s, 0, j)
        @pl.when(s == 0)
        def _():
            for later in range(lines):
                pass_all(later, (3,))

        need(s, 2)
        for j in streams:
            feed(s, j)
            if j == 0:
                need(s, 3)
            leave_feed(s, j)


        @pl.when(s >= 2)
        def _():
            forward_rows(s - 2)


        @pl.when(s + 1 < lines)
        def _():
            small_ready(s + 1)

        for j in streams:
            finish(s, j)
            scatter_sent(s, 1, j)

            @pl.when(s + 1 < lines)
            def _():
                enter(s + 1, j)

        home_start(out_home, s)

        @pl.when(s == 0)
        def _():
            pass_far(1, 0)
            pass_far(1, 1)

        return 0

    lax.fori_loop(0, lines, forward, 0)

    @on_owner
    def turn(s, j):
        upstream = r.upstream[j]
        r.ups[s, j, mine] = upstream
        gather_start(r.ups, s, 2, j)
        r.norm_part[s, 5:6] += column_sum(upstream)

    def feed_back(s, j):
        gather_wait(r.ups, s, 2, j)
        grad_pre = (dot_nt(r.ups[s, j], r.wp[s]) * r.slope[s, j]).astype(LOW)
        r.gpre[s, j] = grad_pre
        scatter_start(s, 2, j, dot_nt(grad_pre, r.wf[s]))
        r.norm_part[s, 6:7, :units] += column_sum(grad_pre)
        gather_sent(r.ups, s, 2, j)

    @on_owner
    def between_back(s, j):
        grad = scatter_sum(s, 2, j)
        xhat = r.xhat2[s, j]
        upstream = r.upstream[j].astype(F32)
        grad_middle = upstream + standard_back(
            grad * r.small[s, 2:3], xhat, r.inv2[s, j, :, 0:1]
        )
        r.middle[j] = grad_middle
        branch = grad_middle.astype(LOW)
        r.brn[s, j, mine] = branch
        gather_start(r.brn, s, 3, j)
        r.norm_part[s, 2:3] += column_sum(grad * xhat)
        r.norm_part[s, 3:4] += column_sum(grad)
        r.norm_part[s, 4:5] += column_sum(branch)

    def mixed_back(s, j):
        gather_wait(r.brn, s, 3, j)
        place = place_of(c * local + j * stream_rows + iota((stream_rows, 1), 0))
        r.gmix[j] = (dot_nt(r.brn[s, j], r.wo[s]) * row_mask(place)).astype(LOW)
        gather_sent(r.brn, s, 3, j)

    def attend_line_back(s, j):
        grad_q, grad_k, grad_v = [], [], []
        for head in range(heads):
            cols = head_cols(head)
            weights = r.soft[s, j, head]
            grad_head = r.gmix[j, :, cols]
            grad_weights = dot_nt(grad_head, r.kv[s, 1, :, cols])
            inner = jnp.sum(weights * grad_weights, axis=-1, keepdims=True)
            grad_scores = (weights * (grad_weights - inner)).astype(LOW)
            grad_k.append(scale * dot_tn(grad_scores, r.qry[s, j, :, cols]))
            grad_v.append(dot_tn(weights.astype(LOW), grad_head))
            grad_q.append(scale * dot_nn(grad_scores, r.kv[s, 0, :, cols]))
        for which, grad in enumerate((grad_k, grad_v)):
            grad = jnp.concatenate(grad, axis=-1)
            r.dkv_all[which] = grad if j == 0 else r.dkv_all[which] + grad
        grad_q = jnp.concatenate(grad_q, axis=-1).astype(LOW)
        r.dqkv[s, 0, j] = grad_q
        r.norm_part[s, 7:8, :head_width] += column_sum(grad_q)

    def join_keys(s):
        @pl.when(c == 1)
        def _():
            r.dkv_out[s] = r.dkv_all[:, 0:local].astype(LOW)
            dkv_copy(s).start()

        @pl.when(c == 0)
        def _():
            dkv_copy(s).wait_recv()
            r.dkv_all[:, 0:local] += r.dkv_in[s].astype(F32)

        for which in range(2):
            joined = r.dkv_all[which, my_half].astype(LOW)
            r.dqkv[s, 1 + which] = joined.reshape(r.dqkv.shape[2:])
            if which == 1:
                r.norm_part[s, 7:8, half_width : half_width + head_width] = column_sum(joined)

    def leave_back(s, j):
        product = dot_nn(r.dqkv[s, 0, j], r.wq[s, 0:head_width])
        for which in range(1, 3):
            weight = r.wq[s, which * head_width : (which + 1) * head_width]
            product = product + dot_nn(r.dqkv[s, which, j], weight)
        scatter_start(s, 3, j, product)

    @on_owner
    def finish_back(s, j):
        grad = scatter_sum(s, 3, j)
        xhat = r.xhat1[s, j]
        result = r.middle[j] + standard_back(
            grad * r.small[s, 0:1], xhat, r.inv1[s, j, :, 0:1]
        )
        r.upstream[j] = result.astype(LOW)
        keep_rows(r.grad_low, s, j, result.astype(LOW))
        r.norm_part[s, 0:1] += column_sum(grad * xhat)
        r.norm_part[s, 1:2] += column_sum(grad)

    for j in streams:
        turn(lines - 1, j)

    def backward(index, _):
        s = lines - 1 - index
        for j in streams:
            feed_back(s, j)
        rows_start(UPS, s)
        rows_start(GPRE, s)

        @pl.when(index < 2)
        def _():
            forward_rows(lines - 2 + index)

        @pl.when(index == lines - 1)
        def _():
            share(ACT)
            share(MIX)

        for j in streams:
            between_back(s, j)
            scatter_sent(s, 2, j)
        for j in streams:
            mixed_back(s, j)
            attend_line_back(s, j)
        join_keys(s)
        rows_start(BRN, s)
        for j in streams:
            leave_back(s, j)
        rows_start(DQKV, s)
        for j in streams:
            finish_back(s, j)
            scatter_sent(s, 3, j)

            @pl.when(s > 0)
            def _():
                turn(s - 1, j)

        norm_start(s)
        home_start(grad_home, s)
        return 0

    lax.fori_loop(0, lines, backward, 0)

    share(GPRE)
    share(DQKV)

    drain(r.norm_all, r.norm_r)
    slot = c * chips + t
    norm_sum = r.norm_all[0]
    for line in range(1, lines):
        norm_sum = norm_sum + r.norm_all[line]
    r.ends[slot] = norm_sum

    def ends_copy(step):
        core, chip = step // chips, step % chips
        view = r.ends.at[slot]
        return remote(
            view,
            view,
            r.ends_s.at[step - 1],
            r.ends_r,
            seq=(c + core) % 2,
            tensor=(t + chip) % chips,
        )

    for step in range(1, 2 * chips):
        ends_copy(step).start()

    for index in range(ACT):
        drain(all_rows[index], r.rows_r.at[index])
    for index in range(ACT, 8):
        share_copy(index, 1 - c).wait_recv()
        share_copy(index, c).wait_send()
    drain(r.acts, r.out_r)
    drain(r.grads, r.grad_r)
    drain(r.ends.at[0 : 2 * chips - 1], r.ends_r)
    for step in range(1, 2 * chips):
        ends_copy(step).wait_send()
    for step in range(1, lines):
        small_copy(step - 1, (a + step) % lines, a).wait_send()
        count_copy(step - 1, (a + step) % lines, a).wait_send()
    for p in range(4):
        for which, line in enumerate((beside(a), above(a))):
            first_hop(p, a, line, which).wait_send()

    @pl.when(end_chip)
    def _():
        first_copy().wait_send()

    def sent(s, _):
        home_sent(out_home, s)
        home_sent(grad_home, s)

        @pl.when(a != s)
        def _():
            norm_copy(s).wait_send()

        @pl.when(c == 0)
        def _():
            kv_copy(s).wait_send()

        @pl.when(c == 1)
        def _():
            dkv_copy(s).wait_send()

        for index in range(8):
            rows_sent(index, s)
        for p in range(4):

            @pl.when((a == beside(s)) | (a == above(s)))
            def _():
                second_hop(p, s, 0).wait_send()

            @pl.when(a != s)
            def _():
                core_hop(p, s, c).wait_send()

        return 0

    lax.fori_loop(0, lines, sent, 0)


def relay_call(inputs, cotangent, lengths, chosen, singles, weights):
    lines = lax.axis_size("section")
    chips = lax.axis_size("tensor")
    rows, buckets, width = inputs.shape[1:]
    local, total, half = rows * chips, 2 * rows * chips, width // 2
    head_width, units = weights["wo_in"].shape[0], weights["wp_in"].shape[0]
    heads = head_width // HDIM
    stream = local // STREAMS
    peers, owned = chips - 1, stream // 2
    vmem, dma = pltpu.VMEM, pltpu.SemaphoreType.DMA
    operands = dict(
        inputs=inputs,
        cotangent=cotangent,
        lengths=lengths,
        chosen=chosen,
        **singles,
        **weights,
    )

    def space(name):
        if name in weights:
            return pl.ANY
        return pltpu.SMEM if operands[name] is lengths else pltpu.VMEM

    sums = dict(
        acts=((lines, rows, width), LOW),
        grads=((lines, rows, width), LOW),
        ends=((2 * chips, 8, width), F32),
    )
    gathered = dict(
        all_nrm=((lines, 2, STREAMS, stream, half), LOW),
        all_nmlp=((lines, 2, STREAMS, stream, half), LOW),
        all_ups=((lines, 2, STREAMS, stream, half), LOW),
        all_brn=((lines, 2, STREAMS, stream, half), LOW),
        all_act=((lines, 2, STREAMS, stream, units), LOW),
        all_gpre=((lines, 2, STREAMS, stream, units), LOW),
        all_mix=((lines, 2, STREAMS, stream, head_width), LOW),
        all_dqkv=((lines, 2, 3, STREAMS, stream, head_width), LOW),
    )
    outputs = dict(**sums, **gathered)
    scratch = dict(
        wq=vmem((lines,) + weights["wq_in"].shape, LOW),
        wo=vmem((lines,) + weights["wo_in"].shape, LOW),
        wf=vmem((lines,) + weights["wf_in"].shape, LOW),
        wp=vmem((lines,) + weights["wp_in"].shape, LOW),
        small_own=vmem((8, width), F32),
        small=vmem((lines, 8, width), F32),
        count_own=vmem((lines, 8, total), F32),
        count=vmem((lines, 8, total), F32),
        hidden=vmem((STREAMS, owned, width), F32),
        middle=vmem((STREAMS, owned, width), F32),
        upstream=vmem((STREAMS, owned, width), LOW),
        first_out=vmem((2, rows, width), LOW),
        first_in=vmem((2, rows, width), LOW),
        xhat1=vmem((lines, STREAMS, owned, width), F32),
        inv1=vmem((lines, STREAMS, owned, 128), F32),
        xhat2=vmem((lines, STREAMS, owned, width), F32),
        inv2=vmem((lines, STREAMS, owned, 128), F32),
        nrm=vmem((lines, STREAMS, stream, width), LOW),
        nmlp=vmem((lines, STREAMS, stream, width), LOW),
        ups=vmem((lines, STREAMS, stream, width), LOW),
        brn=vmem((lines, STREAMS, stream, width), LOW),
        act=vmem((lines, STREAMS, stream, units), LOW),
        gpre=vmem((lines, STREAMS, stream, units), LOW),
        slope=vmem((lines, STREAMS, stream, units), F32),
        mix=vmem((lines, STREAMS, stream, head_width), LOW),
        qry=vmem((lines, STREAMS, stream, head_width), LOW),
        gmix=vmem((STREAMS, stream, head_width), LOW),
        dqkv=vmem((lines, 3, STREAMS, stream, head_width), LOW),
        kv=vmem((lines, 2, total, head_width), LOW),
        soft=vmem((lines, STREAMS, heads, stream, total), F32),
        near=vmem((STREAMS, stream, total), F32),
        dkv_all=vmem((2, total, head_width), F32),
        dkv_out=vmem((lines, 2, local, head_width), LOW),
        dkv_in=vmem((lines, 2, local, head_width), LOW),
        part=vmem((4, STREAMS, stream, width), LOW),
        arrived=vmem((lines, 4, STREAMS, peers, owned, width), LOW),
        out_low=vmem((lines, 2, rows, width), LOW),
        grad_low=vmem((lines, 2, rows, width), LOW),
        norm_part=vmem((lines, 8, width), F32),
        norm_all=vmem((lines, 8, width), F32),
        w_first_s=dma((4, 2)),
        w_first_r=dma((lines, 4)),
        w_second_s=dma((lines, 4)),
        w_second_r=dma((lines, 4, 2)),
        w_core_s=dma((lines, 4)),
        w_core_r=dma((lines, 4)),
        w_own=dma((4,)),
        small_s=dma((lines - 1,)),
        small_r=dma((lines,)),
        count_s=dma((lines - 1,)),
        count_r=dma((lines,)),
        ag_s=dma((4, STREAMS, peers)),
        ag_r=dma((4, STREAMS, peers)),
        rs_s=dma((4, STREAMS, peers)),
        rs_r=dma((4, STREAMS, peers)),
        kv_s=dma((lines,)),
        kv_r=dma((lines,)),
        dkv_s=dma((lines,)),
        dkv_r=dma((lines,)),
        rows_s=dma((8, lines, 2)),
        rows_r=dma((8,)),
        share_s=dma((4,)),
        share_r=dma((4,)),
        first_s=dma,
        first_r=dma,
        out_s=dma((lines, 2)),
        out_r=dma,
        grad_s=dma((lines, 2)),
        grad_r=dma,
        norm_s=dma((lines,)),
        norm_r=dma,
        ends_s=dma((2 * chips - 1,)),
        ends_r=dma,
    )
    names = tuple(operands) + tuple(outputs) + tuple(scratch)
    results = pl.pallas_call(
        functools.partial(relay_kernel, names),
        out_shape=[jax.ShapeDtypeStruct(shape, kind) for shape, kind in outputs.values()],
        in_specs=[pl.BlockSpec(memory_space=space(name)) for name in operands],
        out_specs=[
            pl.BlockSpec(memory_space=pl.ANY if name in gathered else pltpu.VMEM)
            for name in outputs
        ],
        scratch_shapes=list(scratch.values()),
        compiler_params=pltpu.CompilerParams(
            collective_id=0, has_side_effects=True, vmem_limit_bytes=60 * 2**20
        ),
        name="relay",
    )(*operands.values())
    return dict(zip(outputs, results))


def weights_kernel(names, *refs):
    r = types.SimpleNamespace(**dict(zip(names, refs)))
    step = pl.program_id(0)
    micro_count, rows, buckets, width = r.activations.shape
    chips, units, head_width = r.ends.shape[0] // 2, r.all_act.shape[-1], r.all_mix.shape[-1]

    @pl.when(step == 0)
    def _():
        sums = r.ends[0]
        for other in range(1, 2 * chips):
            sums = sums + r.ends[other]
        singles = (r.ln1_gain, r.ln1_shift, r.ln2_gain, r.ln2_shift, r.b_out, r.b_proj)
        for place, single in enumerate(singles):
            single[...] = sums[place : place + 1]
        for chip in range(chips):
            both = r.ends[chip] + r.ends[chips + chip]
            r.b_fc[:, chip * units : (chip + 1) * units] = both[6:7, :units]
            here = slice(chip * head_width, (chip + 1) * head_width)
            r.b_qv[0:1, here] = both[7:8, :head_width]
            r.b_qv[1:2, here] = both[7:8, width // 2 : width // 2 + head_width]
        for target, source in ((r.activations, r.acts), (r.in_grads, r.grads)):
            for micro in range(micro_count):
                rows_of = [
                    source[micro * buckets + bucket].astype(F32)[:, None, :]
                    for bucket in range(buckets)
                ]
                target[micro] = jnp.concatenate(rows_of, axis=1).astype(LOW)
        for target in (r.w_qkv, r.w_out, r.w_fc, r.w_proj):
            target[...] = jnp.zeros_like(target)

    def rows_of_sequence(ref):
        return ref[0].reshape(2 * chips * rows, ref.shape[-1])

    nrm, nmlp, ups, brn, act, gpre, mix = (
        rows_of_sequence(ref)
        for ref in (r.all_nrm, r.all_nmlp, r.all_ups, r.all_brn, r.all_act, r.all_gpre, r.all_mix)
    )
    r.w_proj[...] += dot_tn(act, ups)
    r.w_fc[...] += dot_tn(nmlp, gpre)
    r.w_out[...] += dot_tn(mix, brn)
    for which in range(3):
        grad = r.all_dqkv[0, :, which].reshape(2 * chips * rows, head_width)
        r.w_qkv[which] += dot_tn(grad, nrm)


def weights_call(relayed, inputs_shape, head_width, units):
    lines = lax.axis_size("section")
    chips = lax.axis_size("tensor")
    width = inputs_shape[-1]
    half = width // 2
    outputs = dict(
        activations=(inputs_shape, LOW),
        in_grads=(inputs_shape, LOW),
        ln1_gain=((1, width), F32),
        ln1_shift=((1, width), F32),
        w_qkv=((3, head_width, half), F32),
        b_qv=((2, width), F32),
        w_out=((head_width, half), F32),
        b_out=((1, width), F32),
        ln2_gain=((1, width), F32),
        ln2_shift=((1, width), F32),
        w_fc=((half, units), F32),
        b_fc=((1, chips * units), F32),
        w_proj=((units, half), F32),
        b_proj=((1, width), F32),
    )

    def spec(array):
        if len(array.shape) < 5:
            return pl.BlockSpec(array.shape, lambda step: (0,) * len(array.shape))
        return pl.BlockSpec(
            (1,) + array.shape[1:], lambda step: (step,) + (0,) * (len(array.shape) - 1)
        )

    def whole(shape):
        return pl.BlockSpec(shape, lambda step: (0,) * len(shape))

    return pl.pallas_call(
        functools.partial(weights_kernel, tuple(relayed) + tuple(outputs)),
        out_shape=[jax.ShapeDtypeStruct(shape, kind) for shape, kind in outputs.values()],
        grid=(lines,),
        in_specs=[spec(array) for array in relayed.values()],
        out_specs=[whole(shape) for shape, _ in outputs.values()],
        compiler_params=pltpu.CompilerParams(vmem_limit_bytes=60 * 2**20),
        name="weight_gradients",
    )(*relayed.values())


def on_line(
    inputs,
    cotangent,
    lengths,
    chosen,
    ln1_gain,
    ln1_shift,
    w_qkv,
    b_qv,
    w_out,
    b_out,
    ln2_gain,
    ln2_shift,
    w_fc,
    b_fc,
    w_proj,
    b_proj,
):
    head_width, units = w_out.shape[1], w_fc.shape[2]
    singles = dict(
        ln1_gain=ln1_gain,
        ln1_shift=ln1_shift,
        ln2_gain=ln2_gain,
        ln2_shift=ln2_shift,
        b_out=b_out,
        b_proj=b_proj,
        b_fc=b_fc,
        b_qv=b_qv[0],
    )
    weights = dict(
        wq_in=jnp.swapaxes(w_qkv[0], 1, 2).reshape(-1, inputs.shape[-1]),
        wo_in=w_out[0],
        wf_in=w_fc[0],
        wp_in=w_proj[0],
    )
    picks = chosen.reshape((-1,) + chosen.shape[-2:])
    relayed = relay_call(inputs, cotangent, lengths, picks, singles, weights)
    results = list(weights_call(relayed, inputs.shape, head_width, units))
    results[4] = jnp.swapaxes(results[4], 1, 2)
    vectors = (2, 3, 7, 8, 9, 11, 13)
    return tuple(
        result if place in vectors else result[None] for place, result in enumerate(results)
    )


def fits_lines(mesh):
    return mesh.shape["section"] == 4 and mesh.shape["seq"] == 2 and mesh.shape["tensor"] == 4


def solution(mesh):
    placed = (
        P(None, ("seq", "tensor"), None, None),
        P(None, ("seq", "tensor"), None, None),
        P(),
        P("section", None, None, "tensor", "seq", None),
        P("section", None),
        P("section", None),
        P("section", None, None, "tensor"),
        P("section", None, "tensor"),
        P("section", "tensor", None),
        P("section", None),
        P("section", None),
        P("section", None),
        P("section", None, "tensor"),
        P("section", "tensor"),
        P("section", "tensor", None),
        P("section", None),
    )
    return jax.shard_map(
        on_line if fits_lines(mesh) else on_device,
        mesh=mesh,
        in_specs=placed,
        out_specs=(
            P("section", None, ("seq", "tensor"), None, None),
            P("section", None, ("seq", "tensor"), None, None),
            P("section", None),
            P("section", None),
            P("section", None, "seq", "tensor"),
            P("section", None, None),
            P("section", "tensor", "seq"),
            P("section", None),
            P("section", None),
            P("section", None),
            P("section", "seq", "tensor"),
            P("section", None),
            P("section", "tensor", "seq"),
            P("section", None),
        ),
        check_vma=False,
    )
```

```python
import functools
import types

import jax
import jax.numpy as jnp
from jax import lax
from jax.experimental import pallas as pl
from jax.experimental.pallas import tpu as pltpu
from jax.sharding import PartitionSpec as P

HDIM = 64
WIN = 64
QB = 64
KSEL = 64


NORM_EPS = 1e-05
MASKED = -1000000000.0


def from_behind(value, axis, steps):
    count = lax.axis_size(axis)
    first, last = (max(0, -steps), min(count, count - steps))
    return lax.ppermute(value, axis, [(source, source + steps) for source in range(first, last)])


def layer_norm(values, gain, shift):
    average = jnp.mean(values, axis=-1, keepdims=True)
    centred = values - average
    variance = jnp.mean(centred * centred, axis=-1, keepdims=True)
    return centred * lax.rsqrt(variance + NORM_EPS) * gain + shift


def gelu_tanh(values):
    return (
        0.5
        * values
        * (1.0 + jnp.tanh(0.7978845608028654 * (values + 0.044715 * values * values * values)))
    )


def gather_rows(row_block):
    return lax.all_gather(row_block, "tensor", axis=0, tiled=True)


def scatter_product(left_rows, weight, formula):
    return lax.psum_scatter(
        jnp.einsum(formula, left_rows, weight, preferred_element_type=jnp.float32).astype(
            jnp.bfloat16
        ),
        "tensor",
        scatter_dimension=0,
        tiled=True,
    ).astype(jnp.float32)


def near_slabs(full_rows, seq_start, seq_first, length_local):
    buckets = full_rows.shape[1]
    heads_local = full_rows.shape[2] // HDIM
    blocks = length_local // QB
    earlier = lax.dynamic_slice_in_dim(full_rows, jnp.maximum(seq_start - WIN, 0), WIN, 0)
    earlier = jnp.where(seq_first, jnp.zeros_like(earlier), earlier)
    local_part = lax.dynamic_slice_in_dim(full_rows, seq_start, length_local, 0)
    segment = jnp.concatenate([earlier, local_part], 0).reshape(
        length_local + WIN, buckets, heads_local, HDIM
    )
    return jnp.concatenate(
        [
            segment[offset_index * QB : offset_index * QB + length_local].reshape(
                blocks, QB, buckets, heads_local, HDIM
            )
            for offset_index in range(WIN // QB + 1)
        ],
        1,
    )


def far_rows(full_rows, flat_index):
    total_rows, buckets, feature_width = full_rows.shape
    heads_local = feature_width // HDIM
    return jnp.take(full_rows.reshape(total_rows * buckets * heads_local, HDIM), flat_index, axis=0)


def key_geometry(chosen_now, seq_start, blocks):
    buckets, heads_local = (chosen_now.shape[0], chosen_now.shape[1])
    bucket_ids = lax.broadcasted_iota(jnp.int32, chosen_now.shape, 0)
    head_ids = lax.broadcasted_iota(jnp.int32, chosen_now.shape, 1)
    flat_index = (chosen_now * buckets + bucket_ids) * heads_local + head_ids
    block_start = seq_start + QB * lax.broadcasted_iota(jnp.int32, (blocks, 1, 1), 0)
    query_ids = lax.broadcasted_iota(jnp.int32, (1, QB, 1), 1)
    key_ids = lax.broadcasted_iota(jnp.int32, (1, 1, WIN + QB), 2)
    distance = query_ids + WIN - key_ids
    near_ok = (distance >= 0) & (distance < WIN) & (block_start + key_ids - WIN >= 0)
    far_ok = chosen_now + WIN <= block_start.reshape(1, 1, blocks, 1)
    near_mask = jnp.broadcast_to(
        near_ok[:, None, None], (blocks, buckets, heads_local, QB, WIN + QB)
    )
    far_mask = jnp.broadcast_to(
        jnp.transpose(far_ok, (2, 0, 1, 3))[:, :, :, None, :],
        (blocks, buckets, heads_local, QB, KSEL),
    )
    return (flat_index, jnp.concatenate([near_mask, far_mask], -1))


def attention_setup(queries, key_rows, value_rows, chosen_now, seq_start, seq_first):
    length_local, buckets, feature_width = queries.shape
    heads_local = feature_width // HDIM
    blocks = length_local // QB
    query_blocks = queries.reshape(blocks, QB, buckets, heads_local, HDIM)
    flat_index, key_mask = key_geometry(chosen_now, seq_start, blocks)
    near_keys = near_slabs(key_rows, seq_start, seq_first, length_local)
    near_values = near_slabs(value_rows, seq_start, seq_first, length_local)
    far_keys = far_rows(key_rows, flat_index)
    far_values = far_rows(value_rows, flat_index)
    near_scores = jnp.einsum(
        "bqnhe,btnhe->bnhqt", query_blocks, near_keys, preferred_element_type=jnp.float32
    )
    far_scores = jnp.einsum(
        "bqnhe,nhbke->bnhqk", query_blocks, far_keys, preferred_element_type=jnp.float32
    )
    scores = jnp.where(
        key_mask, HDIM ** (-0.5) * jnp.concatenate([near_scores, far_scores], -1), MASKED
    )
    return (query_blocks, near_keys, near_values, far_keys, far_values, flat_index, scores)


def attend(queries, key_rows, value_rows, chosen_now, seq_start, seq_first):
    query_blocks, near_keys, near_values, far_keys, far_values, flat_index, scores = (
        attention_setup(queries, key_rows, value_rows, chosen_now, seq_start, seq_first)
    )
    span = WIN + QB
    row_top = jnp.max(scores, -1, keepdims=True)
    exp_terms = jnp.exp(scores - row_top)
    row_total = jnp.sum(exp_terms, -1, keepdims=True)
    softmax_low = (exp_terms / row_total).astype(jnp.bfloat16)
    near_part = jnp.einsum(
        "bnhqt,btnhe->bqnhe",
        softmax_low[..., :span],
        near_values,
        preferred_element_type=jnp.float32,
    )
    far_part = jnp.einsum(
        "bnhqk,nhbke->bqnhe",
        softmax_low[..., span:],
        far_values,
        preferred_element_type=jnp.float32,
    )
    return ((near_part + far_part).reshape(queries.shape), row_top + jnp.log(row_total))


def spread_back(near_grad, far_grad, flat_index, seq_start, seq_first, total_rows):
    blocks, span, buckets, heads_local, head_size = near_grad.shape
    length_local = blocks * QB
    feature_width = heads_local * head_size
    segment = jnp.zeros((length_local + WIN, buckets, heads_local, head_size), jnp.float32)
    for offset_index in range(WIN // QB + 1):
        piece = near_grad[:, offset_index * QB : (offset_index + 1) * QB].reshape(
            length_local, buckets, heads_local, head_size
        )
        segment = segment.at[offset_index * QB : offset_index * QB + length_local].add(piece)
    full_rows = jnp.zeros((total_rows * buckets * heads_local, head_size), jnp.float32)
    full_rows = full_rows.at[flat_index.reshape(-1)].add(far_grad.reshape(-1, head_size))
    full_rows = full_rows.reshape(total_rows, buckets, feature_width)
    local_part = segment[WIN:].reshape(length_local, buckets, feature_width)
    earlier = jnp.where(seq_first, 0.0, segment[:WIN].reshape(WIN, buckets, feature_width))
    full_rows = lax.dynamic_update_slice_in_dim(
        full_rows,
        lax.dynamic_slice_in_dim(full_rows, seq_start, length_local, 0) + local_part,
        seq_start,
        0,
    )
    earlier_start = jnp.maximum(seq_start - WIN, 0)
    full_rows = lax.dynamic_update_slice_in_dim(
        full_rows,
        lax.dynamic_slice_in_dim(full_rows, earlier_start, WIN, 0) + earlier,
        earlier_start,
        0,
    )
    return full_rows


def attend_back(
    queries, key_rows, value_rows, chosen_now, seq_start, seq_first, log_total, grad_mixed
):
    query_blocks, near_keys, near_values, far_keys, far_values, flat_index, scores = (
        attention_setup(queries, key_rows, value_rows, chosen_now, seq_start, seq_first)
    )
    span = WIN + QB
    score_scale = HDIM ** (-0.5)
    grad_blocks = grad_mixed.reshape(query_blocks.shape)
    weights_full = jnp.exp(scores - log_total)
    softmax_low = weights_full.astype(jnp.bfloat16)
    grad_near_weights = jnp.einsum(
        "bqnhe,btnhe->bnhqt", grad_blocks, near_values, preferred_element_type=jnp.float32
    )
    grad_far_weights = jnp.einsum(
        "bqnhe,nhbke->bnhqk", grad_blocks, far_values, preferred_element_type=jnp.float32
    )
    grad_weights = jnp.concatenate([grad_near_weights, grad_far_weights], -1)
    row_dot = jnp.sum(weights_full * grad_weights, -1, keepdims=True)
    grad_scores = (weights_full * (grad_weights - row_dot)).astype(jnp.bfloat16)
    grad_near, grad_far = (grad_scores[..., :span], grad_scores[..., span:])
    grad_queries = score_scale * (
        jnp.einsum("bnhqt,btnhe->bqnhe", grad_near, near_keys, preferred_element_type=jnp.float32)
        + jnp.einsum("bnhqk,nhbke->bqnhe", grad_far, far_keys, preferred_element_type=jnp.float32)
    )
    near_key_grad = score_scale * jnp.einsum(
        "bnhqt,bqnhe->btnhe", grad_near, query_blocks, preferred_element_type=jnp.float32
    )
    far_key_grad = score_scale * jnp.einsum(
        "bnhqk,bqnhe->nhbke", grad_far, query_blocks, preferred_element_type=jnp.float32
    )
    near_value_grad = jnp.einsum(
        "bnhqt,bqnhe->btnhe",
        softmax_low[..., :span],
        grad_blocks,
        preferred_element_type=jnp.float32,
    )
    far_value_grad = jnp.einsum(
        "bnhqk,bqnhe->nhbke",
        softmax_low[..., span:],
        grad_blocks,
        preferred_element_type=jnp.float32,
    )
    total_rows = key_rows.shape[0]
    key_grad = spread_back(
        near_key_grad, far_key_grad, flat_index, seq_start, seq_first, total_rows
    )
    value_grad = spread_back(
        near_value_grad, far_value_grad, flat_index, seq_start, seq_first, total_rows
    )
    return (grad_queries.reshape(queries.shape), key_grad, value_grad)


def forward_pass(hidden, params, chosen_now, query_mask, seq_start, seq_first, finish):
    (
        ln1_gain,
        ln1_shift,
        w_qkv,
        b_qv,
        w_out,
        b_out,
        ln2_gain,
        ln2_shift,
        w_fc,
        b_fc,
        w_proj,
        b_proj,
    ) = params
    hidden_wide = hidden.astype(jnp.float32)
    normed_all = gather_rows(layer_norm(hidden_wide, ln1_gain, ln1_shift).astype(jnp.bfloat16))
    projected = jnp.einsum("pnd,jdc->jpnc", normed_all, w_qkv, preferred_element_type=jnp.float32)
    queries = (projected[0] + b_qv[0]).astype(jnp.bfloat16)
    key_rows, value_rows = (
        lax.all_gather(projected[1].astype(jnp.bfloat16), "seq", axis=0, tiled=True),
        lax.all_gather((projected[2] + b_qv[1]).astype(jnp.bfloat16), "seq", axis=0, tiled=True),
    )
    attended, log_total = attend(queries, key_rows, value_rows, chosen_now, seq_start, seq_first)
    mixed_rows = (attended * query_mask[:, :, None]).astype(jnp.bfloat16)
    middle = hidden_wide + scatter_product(mixed_rows, w_out, "pnc,cd->pnd") + b_out
    normed_mlp = gather_rows(layer_norm(middle, ln2_gain, ln2_shift).astype(jnp.bfloat16))
    pre_active = (
        jnp.einsum("pnd,df->pnf", normed_mlp, w_fc, preferred_element_type=jnp.float32) + b_fc
    )
    active = gelu_tanh(pre_active).astype(jnp.bfloat16)
    if not finish:
        return (
            normed_all,
            queries,
            key_rows,
            value_rows,
            log_total,
            mixed_rows,
            middle,
            normed_mlp,
            pre_active,
            active,
        )
    output = (middle + scatter_product(active, w_proj, "pnf,fd->pnd") + b_proj).astype(jnp.bfloat16)
    return (output, (key_rows, value_rows))


def backward_pass(hidden, upstream, params, chosen_now, query_mask, seq_start, seq_first):
    (
        ln1_gain,
        ln1_shift,
        w_qkv,
        b_qv,
        w_out,
        b_out,
        ln2_gain,
        ln2_shift,
        w_fc,
        b_fc,
        w_proj,
        b_proj,
    ) = params
    (
        normed_all,
        queries,
        key_rows,
        value_rows,
        log_total,
        mixed_rows,
        middle,
        normed_mlp,
        pre_active,
        active,
    ) = forward_pass(hidden, params, chosen_now, query_mask, seq_start, seq_first, False)
    upstream_all = gather_rows(upstream)
    grad_w_proj = jnp.einsum(
        "pnf,pnd->fd", active, upstream_all, preferred_element_type=jnp.float32
    )
    grad_b_proj = jnp.sum(upstream.astype(jnp.float32), axis=(0, 1))
    grad_active = jnp.einsum(
        "pnd,fd->pnf", upstream_all, w_proj, preferred_element_type=jnp.float32
    )
    unused_value, gelu_pull = jax.vjp(gelu_tanh, pre_active)
    grad_pre = gelu_pull(grad_active)[0].astype(jnp.bfloat16)
    grad_w_fc = jnp.einsum("pnd,pnf->df", normed_mlp, grad_pre, preferred_element_type=jnp.float32)
    grad_b_fc = jnp.sum(grad_pre.astype(jnp.float32), axis=(0, 1))
    grad_normed_mlp = scatter_product(grad_pre, w_fc, "pnf,df->pnd")
    unused_norm, second_pull = jax.vjp(layer_norm, middle, ln2_gain, ln2_shift)
    grad_mid_norm, grad_ln2_gain, grad_ln2_shift = second_pull(grad_normed_mlp)
    grad_middle = upstream.astype(jnp.float32) + grad_mid_norm
    grad_branch = grad_middle.astype(jnp.bfloat16)
    grad_b_out = jnp.sum(grad_branch.astype(jnp.float32), axis=(0, 1))
    branch_all = gather_rows(grad_branch)
    grad_w_out = jnp.einsum(
        "pnc,pnd->cd", mixed_rows, branch_all, preferred_element_type=jnp.float32
    )
    grad_mixed = jnp.einsum(
        "pnd,cd->pnc", branch_all, w_out, preferred_element_type=jnp.float32
    ).astype(jnp.bfloat16) * query_mask[:, :, None].astype(jnp.bfloat16)
    grad_queries, key_grad_all, value_grad_all = attend_back(
        queries, key_rows, value_rows, chosen_now, seq_start, seq_first, log_total, grad_mixed
    )
    key_grad, value_grad = (
        lax.psum_scatter(
            key_grad_all.astype(jnp.bfloat16), "seq", scatter_dimension=0, tiled=True
        ).astype(jnp.float32),
        lax.psum_scatter(
            value_grad_all.astype(jnp.bfloat16), "seq", scatter_dimension=0, tiled=True
        ).astype(jnp.float32),
    )
    grad_project = jnp.stack(
        [
            grad_queries.astype(jnp.bfloat16),
            key_grad.astype(jnp.bfloat16),
            value_grad.astype(jnp.bfloat16),
        ],
        2,
    )
    grad_w_qkv = jnp.einsum(
        "pnd,pnjc->jdc", normed_all, grad_project, preferred_element_type=jnp.float32
    )
    grad_b_qv = jnp.sum(grad_project[:, :, 0::2].astype(jnp.float32), axis=(0, 1))
    grad_normed = scatter_product(grad_project, w_qkv, "pnjc,jdc->pnd")
    unused_first, first_pull = jax.vjp(layer_norm, hidden.astype(jnp.float32), ln1_gain, ln1_shift)
    grad_in_norm, grad_ln1_gain, grad_ln1_shift = first_pull(grad_normed)
    grad_hidden = (grad_middle + grad_in_norm).astype(jnp.bfloat16)
    block_grads = (
        grad_ln1_gain,
        grad_ln1_shift,
        grad_w_qkv,
        grad_b_qv,
        grad_w_out,
        grad_b_out,
        grad_ln2_gain,
        grad_ln2_shift,
        grad_w_fc,
        grad_b_fc,
        grad_w_proj,
        grad_b_proj,
    )
    return (grad_hidden, block_grads)


def on_device(
    inputs,
    cotangent,
    lengths,
    chosen,
    ln1_gain,
    ln1_shift,
    w_qkv,
    b_qv,
    w_out,
    b_out,
    ln2_gain,
    ln2_shift,
    w_fc,
    b_fc,
    w_proj,
    b_proj,
):
    params = tuple(
        (
            weight_array[0]
            for weight_array in (
                ln1_gain,
                ln1_shift,
                w_qkv,
                b_qv,
                w_out,
                b_out,
                ln2_gain,
                ln2_shift,
                w_fc,
                b_fc,
                w_proj,
                b_proj,
            )
        )
    )
    section_index = lax.axis_index("section")
    section_count = lax.axis_size("section")
    seq_index = lax.axis_index("seq")
    tensor_index = lax.axis_index("tensor")
    tensor_count = lax.axis_size("tensor")
    micro_count, rows_local, buckets, feature_width = inputs.shape
    length_local = rows_local * tensor_count
    heads_width = w_qkv.shape[-1]
    seq_start = seq_index * length_local
    seq_first = seq_index == 0
    positions = seq_start + lax.broadcasted_iota(jnp.int32, (micro_count, length_local, buckets), 1)
    mask_all = (positions < lengths[:, None, :]).astype(jnp.float32)
    mask_rows = lax.dynamic_slice_in_dim(mask_all, tensor_index * rows_local, rows_local, 1)
    step_count = micro_count + section_count - 1
    chosen_section = chosen[0]
    received = jnp.zeros((rows_local, buckets, feature_width), jnp.bfloat16)
    stored = jnp.zeros((micro_count, rows_local, buckets, feature_width), jnp.bfloat16)
    outputs = jnp.zeros_like(stored)
    for step_index in range(step_count):
        micro_index = step_index - section_index
        running = (micro_index >= 0) & (micro_index < micro_count)
        slot_index = jnp.clip(micro_index, 0, micro_count - 1)
        block_in = jnp.where(
            section_index == 0, lax.dynamic_index_in_dim(inputs, slot_index, 0, False), received
        )
        chosen_now = lax.dynamic_index_in_dim(chosen_section, slot_index, 0, False)
        query_mask = lax.dynamic_index_in_dim(mask_all, slot_index, 0, False)
        result, key_pair = forward_pass(
            block_in, params, chosen_now, query_mask, seq_start, seq_first, True
        )
        stored = jnp.where(
            running, lax.dynamic_update_index_in_dim(stored, block_in, slot_index, 0), stored
        )
        outputs = jnp.where(
            running, lax.dynamic_update_index_in_dim(outputs, result, slot_index, 0), outputs
        )
        received = from_behind(result, "section", 1)
    back_received = jnp.zeros((rows_local, buckets, feature_width), jnp.bfloat16)
    in_grads = jnp.zeros_like(stored)
    totals = None
    for step_index in range(step_count):
        micro_index = step_index - (section_count - 1 - section_index)
        running = (micro_index >= 0) & (micro_index < micro_count)
        slot_index = jnp.clip(micro_index, 0, micro_count - 1)
        chosen_now = lax.dynamic_index_in_dim(chosen_section, slot_index, 0, False)
        query_mask = lax.dynamic_index_in_dim(mask_all, slot_index, 0, False)
        local_mask = lax.dynamic_index_in_dim(mask_rows, slot_index, 0, False)
        top_grad = (
            lax.dynamic_index_in_dim(cotangent, slot_index, 0, False).astype(jnp.float32)
            * local_mask[:, :, None]
        ).astype(jnp.bfloat16)
        upstream = jnp.where(section_index == section_count - 1, top_grad, back_received)
        hidden = lax.dynamic_index_in_dim(stored, slot_index, 0, False)
        grad_hidden, block_grads = backward_pass(
            hidden, upstream, params, chosen_now, query_mask, seq_start, seq_first
        )
        block_grads = tuple(
            (jnp.where(running, grad_part, jnp.zeros_like(grad_part)) for grad_part in block_grads)
        )
        totals = (
            block_grads
            if step_index == 0
            else tuple(
                (total_part + grad_part for total_part, grad_part in zip(totals, block_grads))
            )
        )
        in_grads = jnp.where(
            running, lax.dynamic_update_index_in_dim(in_grads, grad_hidden, slot_index, 0), in_grads
        )
        back_received = from_behind(grad_hidden, "section", -1)
    (
        sum_ln1_gain,
        sum_ln1_shift,
        sum_w_qkv,
        sum_b_qv,
        sum_w_out,
        sum_b_out,
        sum_ln2_gain,
        sum_ln2_shift,
        sum_w_fc,
        sum_b_fc,
        sum_w_proj,
        sum_b_proj,
    ) = totals
    part_qkv, part_out, part_fc, part_proj = (
        lax.psum_scatter(
            sum_w_qkv.astype(jnp.bfloat16), "seq", scatter_dimension=1, tiled=True
        ).astype(jnp.float32),
        lax.psum_scatter(
            sum_w_out.astype(jnp.bfloat16), "seq", scatter_dimension=1, tiled=True
        ).astype(jnp.float32),
        lax.psum_scatter(
            sum_w_fc.astype(jnp.bfloat16), "seq", scatter_dimension=0, tiled=True
        ).astype(jnp.float32),
        lax.psum_scatter(
            sum_w_proj.astype(jnp.bfloat16), "seq", scatter_dimension=1, tiled=True
        ).astype(jnp.float32),
    )
    bias_qv = lax.dynamic_update_slice_in_dim(
        jnp.zeros((2, feature_width), jnp.float32), sum_b_qv, tensor_index * heads_width, 1
    )
    units_local = sum_b_fc.shape[0]
    bias_fc = lax.dynamic_update_slice_in_dim(
        jnp.zeros((units_local * tensor_count,), jnp.float32),
        sum_b_fc,
        tensor_index * units_local,
        0,
    )
    small_sums = lax.psum(
        (
            sum_ln1_gain,
            sum_ln1_shift,
            bias_qv,
            sum_b_out,
            sum_ln2_gain,
            sum_ln2_shift,
            bias_fc,
            sum_b_proj,
        ),
        ("seq", "tensor"),
    )
    return (
        outputs[None],
        in_grads[None],
        small_sums[0][None],
        small_sums[1][None],
        part_qkv[None],
        small_sums[2][None],
        part_out[None],
        small_sums[3][None],
        small_sums[4][None],
        small_sums[5][None],
        part_fc[None],
        small_sums[6][None],
        part_proj[None],
        small_sums[7][None],
    )


STREAMS = 4
NRM, NMLP, UPS, BRN, ACT, GPRE, MIX, DQKV = range(8)
F32 = jnp.float32
LOW = jnp.bfloat16
MESH_ID = pl.DeviceIdType.MESH


def dot_nn(left, right):
    return lax.dot_general(left, right, (((1,), (0,)), ((), ())), preferred_element_type=F32)


def dot_nt(left, right):
    return lax.dot_general(left, right, (((1,), (1,)), ((), ())), preferred_element_type=F32)


def dot_tn(left, right):
    return lax.dot_general(left, right, (((0,), (0,)), ((), ())), preferred_element_type=F32)


def standard(rows):
    centred = rows - jnp.mean(rows, axis=-1, keepdims=True)
    scale = lax.rsqrt(jnp.mean(centred * centred, axis=-1, keepdims=True) + NORM_EPS)
    return centred * scale, scale


def standard_back(grad, xhat, scale):
    inner = jnp.mean(grad * xhat, axis=-1, keepdims=True)
    return scale * (grad - jnp.mean(grad, axis=-1, keepdims=True) - xhat * inner)


def column_sum(rows):
    return jnp.sum(rows.astype(F32), axis=0, keepdims=True)


def relay_kernel(names, *refs):
    r = types.SimpleNamespace(**dict(zip(names, refs)))
    a, c, t = (lax.axis_index(name) for name in ("section", "seq", "tensor"))
    lines = lax.axis_size("section")
    chips = lax.axis_size("tensor")
    rows, buckets, width = r.inputs.shape[1:]
    half_width = width // 2
    local = rows * chips
    total = 2 * local
    stream_rows = local // STREAMS
    head_width = r.wo_in.shape[0]
    heads = head_width // HDIM
    blocks = local // QB
    units = r.wp_in.shape[0]
    scale = HDIM ** (-0.5)
    streams = range(STREAMS)

    def remote(src, dst, send, recv, **target):
        return pltpu.make_async_remote_copy(
            src_ref=src,
            dst_ref=dst,
            send_sem=send,
            recv_sem=recv,
            device_id=target,
            device_id_type=MESH_ID,
        )

    def drain(ref, sem):
        pltpu.make_async_copy(ref, ref, sem).wait()

    def row_block(index, size):
        return pl.ds(pl.multiple_of(index * size, size), size)

    near_chip = t + 1 - 2 * (t % 2)
    over_chip = (t + 2) % 4
    across_chip = 3 - t
    middle_chip = (t == 1) | (t == 2)
    end_chip = (t == 0) | (t == 3)
    owned = stream_rows // 2
    mine = row_block(t - 1, owned)
    my_half = row_block(c, local)

    r.kv[...] = jnp.zeros(r.kv.shape, LOW)

    barrier = pltpu.get_barrier_semaphore()
    greeted = 0
    for line in range(lines):
        for chip in range(chips):
            for core in range(2):
                if (line, chip, core) != (0, 0, 0) and (core == 0 or line * chip == 0):
                    there = {
                        "section": (a + line) % lines,
                        "seq": (c + core) % 2,
                        "tensor": (t + chip) % chips,
                    }
                    pl.semaphore_signal(barrier, inc=1, device_id=there, device_id_type=MESH_ID)
                    greeted += 1
    pl.semaphore_wait(barrier, greeted)

    def beside(s):
        return s + 1 - 2 * (s % 2)

    def above(s):
        return (s + 2) % 4

    def store(p):
        return (r.wq, r.wo, r.wf, r.wp)[p]

    def source(p):
        return (r.wq_in, r.wo_in, r.wf_in, r.wp_in)[p]

    def height(p):
        return source(p).shape[0]

    def core_half(p, s, core):
        return store(p).at[s, row_block(core, height(p) // 2)]

    def first_hop(p, s, neighbour, which):
        return remote(
            source(p).at[row_block(c, height(p) // 2)],
            core_half(p, s, c),
            r.w_first_s.at[p, which],
            r.w_first_r.at[s, p],
            section=neighbour,
        )

    def second_hop(p, s, which):
        view = store(p).at[s, row_block(2 * c + which, height(p) // 4)]
        return remote(
            view, view, r.w_second_s.at[s, p], r.w_second_r.at[s, p, which], section=3 - s
        )

    def core_hop(p, s, core):
        view = core_half(p, s, core)
        return remote(view, view, r.w_core_s.at[s, p], r.w_core_r.at[s, p], seq=1 - c)

    def own_copy(p):
        return pltpu.make_async_copy(source(p), store(p).at[a], r.w_own.at[p])

    def pass_on(s, p, which):
        line = (beside(s), above(s))[which]

        @pl.when(a == line)
        def _():
            first_hop(p, s, line, which).wait_recv()
            second_hop(p, s, which).start()
            core_hop(p, s, c).start()

    def pass_all(s, pieces):
        for p in pieces:
            for which in range(2):
                pass_on(s, p, which)

    def pass_far(s, p):
        @pl.when(a == 3 - s)
        def _():
            second_hop(p, s, 0).wait_recv()
            second_hop(p, s, 1).wait_recv()
            core_hop(p, s, c).start()

    def need(s, p):
        @pl.when(s == 0)
        def _():
            if p < 2:
                pass_all(0, (p,))
            pass_far(0, p)

        @pl.when(a == s)
        def _():
            own_copy(p).wait()

        @pl.when(a != s)
        def _():
            core_hop(p, s, 1 - c).wait_recv()

    def small_copy(step, line, slot):
        return remote(
            r.small_own, r.small.at[slot], r.small_s.at[step], r.small_r.at[slot], section=line
        )

    def count_copy(step, line, slot):
        return remote(
            r.count_own.at[line],
            r.count.at[slot],
            r.count_s.at[step],
            r.count_r.at[slot],
            section=line,
        )

    singles = (r.ln1_gain, r.ln1_shift, r.ln2_gain, r.ln2_shift, r.b_out, r.b_proj)
    for place, single in enumerate(singles):
        r.small_own[place : place + 1] = single[...]
    r.small_own[6:7, :units] = r.b_fc[...]
    r.small_own[7:8, :head_width] = r.b_qv[0:1]
    r.small_own[7:8, half_width : half_width + head_width] = r.b_qv[1:2]
    for step in range(1, lines):
        small_copy(step - 1, (a + step) % lines, a).start()
    for p in range(4):
        for which, line in enumerate((beside(a), above(a))):
            first_hop(p, a, line, which).start()
    for p in range(4):
        own_copy(p).start()
    r.small[a] = r.small_own[...]

    def iota(shape, dimension):
        return lax.broadcasted_iota(jnp.int32, shape, dimension)

    square = jnp.where(iota((KSEL, KSEL), 0) == iota((KSEL, KSEL), 1), 1.0, 0.0).astype(LOW)
    position = iota((KSEL, total), 1).astype(F32)
    for pair in range(lines * heads):
        line, head = pair // heads, pair % heads
        columns = dot_nt(square, r.chosen[pair].astype(F32).astype(LOW))
        for block in range(blocks):
            pick = head * blocks + block
            r.count_own[line, pick : pick + 1, :] = jnp.sum(
                jnp.where(columns[:, block : block + 1] == position, 1.0, 0.0),
                axis=0,
                keepdims=True,
            )
    for step in range(1, lines):
        count_copy(step - 1, (a + step) % lines, a).start()
    r.count[a] = r.count_own[a]

    NEAR, OVER, ACROSS = range(3)

    def gather(buffer, s, kind, j, owner, target, slot):
        view = buffer.at[s, j, row_block(owner - 1, owned)]
        return remote(
            view, view, r.ag_s.at[kind, j, slot], r.ag_r.at[kind, j, slot], tensor=target
        )

    def gather_start(buffer, s, kind, j):
        gather(buffer, s, kind, j, t, over_chip, OVER).start()
        gather(buffer, s, kind, j, t, across_chip, ACROSS).start()
        gather(buffer, s, kind, j, t, near_chip, NEAR).start()

    def gather_wait(buffer, s, kind, j):
        @pl.when(middle_chip)
        def _():
            gather(buffer, s, kind, j, across_chip, across_chip, ACROSS).wait_recv()

        @pl.when(end_chip)
        def _():
            gather(buffer, s, kind, j, near_chip, near_chip, NEAR).wait_recv()
            gather(buffer, s, kind, j, over_chip, over_chip, OVER).wait_recv()

    def gather_sent(buffer, s, kind, j):
        @pl.when(middle_chip)
        def _():
            gather(buffer, s, kind, j, t, over_chip, OVER).wait_send()
            gather(buffer, s, kind, j, t, across_chip, ACROSS).wait_send()
            gather(buffer, s, kind, j, t, near_chip, NEAR).wait_send()

    def scatter(s, kind, j, owner, slot):
        return remote(
            r.part.at[kind, j, row_block(owner - 1, owned)],
            r.arrived.at[s, kind, j, slot],
            r.rs_s.at[kind, j, slot],
            r.rs_r.at[kind, j, slot],
            tensor=owner,
        )

    def scatter_start(s, kind, j, product):
        r.part[kind, j] = product.astype(LOW)

        @pl.when(end_chip)
        def _():
            scatter(s, kind, j, over_chip, OVER).start()
            scatter(s, kind, j, near_chip, NEAR).start()

        @pl.when(middle_chip)
        def _():
            scatter(s, kind, j, across_chip, ACROSS).start()

    def scatter_sum(s, kind, j):
        result = r.part[kind, j, mine].astype(F32)
        for slot in (NEAR, ACROSS, OVER):
            scatter(s, kind, j, t, slot).wait_recv()
            result = result + r.arrived[s, kind, j, slot].astype(F32)
        return result

    def scatter_sent(s, kind, j):
        @pl.when(end_chip)
        def _():
            scatter(s, kind, j, over_chip, OVER).wait_send()
            scatter(s, kind, j, near_chip, NEAR).wait_send()

        @pl.when(middle_chip)
        def _():
            scatter(s, kind, j, across_chip, ACROSS).wait_send()

    own_rows = (r.nrm, r.nmlp, r.ups, r.brn, r.act, r.gpre, r.mix, r.dqkv)
    all_rows = (
        r.all_nrm,
        r.all_nmlp,
        r.all_ups,
        r.all_brn,
        r.all_act,
        r.all_gpre,
        r.all_mix,
        r.all_dqkv,
    )

    def rows_copy(index, s, same, stays=False):
        core = c if same else 1 - c
        src = own_rows[index].at[s]
        dst = all_rows[index].at[a, c]
        if index <= BRN:
            src = src.at[:, :, row_block(core, half_width)]
        recv = r.rows_r.at[index]
        if stays:
            return pltpu.make_async_copy(src, dst, recv)
        if same:
            return remote(src, dst, r.rows_s.at[index, s, 0], recv, section=s)
        return remote(src, dst, r.rows_s.at[index, s, 1], recv, section=s, seq=1 - c)

    def rows_start(index, s):
        @pl.when(a == s)
        def _():
            rows_copy(index, s, True, True).start()

        @pl.when(a != s)
        def _():
            rows_copy(index, s, True).start()

        if index <= BRN:
            rows_copy(index, s, False).start()

    def forward_rows(s):
        for index in (NRM, MIX, NMLP, ACT):
            rows_start(index, s)

    def rows_sent(index, s):
        @pl.when(a != s)
        def _():
            rows_copy(index, s, True).wait_send()

        if index <= BRN:
            rows_copy(index, s, False).wait_send()

    def share_copy(index, core):
        view = all_rows[index].at[:, core]
        return remote(view, view, r.share_s.at[index - ACT], r.share_r.at[index - ACT], seq=1 - c)

    def share(index):
        drain(all_rows[index].at[:, c], r.rows_r.at[index])
        share_copy(index, c).start()

    def norm_copy(s):
        return remote(
            r.norm_part.at[s], r.norm_all.at[a], r.norm_s.at[s], r.norm_r, section=s
        )

    def norm_start(s):
        @pl.when(a == s)
        def _():
            pltpu.make_async_copy(r.norm_part.at[s], r.norm_all.at[a], r.norm_r).start()

        @pl.when(a != s)
        def _():
            norm_copy(s).start()

    def home_copy(what, s, j, stays=False):
        src, dst, send, recv = what
        view = dst.at[a, mine]
        if stays:
            return pltpu.make_async_copy(src.at[s, j], view, recv)
        return remote(src.at[s, j], view, send.at[s, j], recv, section=s, tensor=j)

    def home_start(what, s):
        for j in streams:
            here = (a == s) & (t == j)

            @pl.when(middle_chip & here)
            def _():
                home_copy(what, s, j, True).start()

            @pl.when(middle_chip & jnp.logical_not(here))
            def _():
                home_copy(what, s, j).start()

    def home_sent(what, s):
        for j in streams:

            @pl.when(middle_chip & ((a != s) | (t != j)))
            def _():
                home_copy(what, s, j).wait_send()

    out_home = (r.out_low, r.acts, r.out_s, r.out_r)
    grad_home = (r.grad_low, r.grads, r.grad_s, r.grad_r)

    length = r.lengths[a // buckets, a % buckets]
    key = iota((stream_rows, total), 1)
    for j in streams:
        query = c * local + j * stream_rows + iota((stream_rows, total), 0)
        r.near[j] = jnp.where((query >= key) & (query - key < WIN), 1.0, 0.0)
    key_row = iota((1, total), 1)

    def row_mask(place):
        return jnp.where(place < length, 1.0, 0.0)

    def stream_mask(j):
        return row_mask(c * local + j * stream_rows + iota((stream_rows, 1), 0))

    def multiplicity(s, j, head):
        block = j * stream_rows // QB
        pick = head * blocks + block
        limit = (c * blocks + block) * QB - WIN
        return r.near[j] + jnp.where(key_row <= limit, r.count[s, pick : pick + 1, :], 0.0)

    def head_cols(head):
        return slice(head * HDIM, (head + 1) * HDIM)

    def kv_copy(s, j):
        view = r.kv.at[s, :, j * stream_rows : (j + 1) * stream_rows]
        return remote(view, view, r.kv_s.at[s, j], r.kv_r.at[s, j], seq=1 - c)

    def dkv_copy(s):
        return remote(r.dkv_out.at[s], r.dkv_in.at[s], r.dkv_s.at[s], r.dkv_r.at[s], seq=1 - c)

    def own_sequence(ref):
        both = ref[a // buckets].astype(F32)
        picked = both[:, 0, :]
        for bucket in range(1, buckets):
            picked = jnp.where(a % buckets == bucket, both[:, bucket, :], picked)
        return picked

    def first_copy(owner, chip):
        return remote(
            r.first_out.at[owner - 1],
            r.first_in.at[chip],
            r.first_s.at[owner - 1],
            r.first_r.at[chip],
            tensor=owner,
        )

    own_place = c * local + t * rows + iota((rows, 1), 0)
    first = (
        own_sequence(r.inputs).astype(LOW),
        (own_sequence(r.cotangent) * row_mask(own_place)).astype(LOW),
    )
    for owner in (1, 2):
        for which in range(2):
            r.first_out[owner - 1, which] = first[which][(owner - 1) * owned : owner * owned]

        @pl.when(t != owner)
        def _():
            first_copy(owner, t).start()

        @pl.when(t == owner)
        def _():
            r.first_in[owner] = r.first_out[owner - 1]

    r.norm_part[...] = jnp.zeros_like(r.norm_part)

    def first_rows(j):
        @pl.when(middle_chip & (t != j))
        def _():
            first_copy(t, j).wait_recv()

        @pl.when(middle_chip)
        def _():
            r.hidden[j] = r.first_in[j, 0].astype(F32)
            r.upstream[j] = r.first_in[j, 1]

    def on_owner(stage):
        def run(s, j):
            @pl.when(middle_chip)
            def _():
                stage(s, j)

        return run

    @on_owner
    def enter(s, j):
        xhat, inverse = standard(r.hidden[j])
        r.xhat1[s, j] = xhat
        r.inv1[s, j] = jnp.broadcast_to(inverse, (owned, 128))
        r.nrm[s, j, mine] = (xhat * r.small[s, 0:1] + r.small[s, 1:2]).astype(LOW)
        gather_start(r.nrm, s, 0, j)

    def project(s, j):
        gather_wait(r.nrm, s, 0, j)
        normed = r.nrm[s, j]
        place = row_block(c * STREAMS + j, stream_rows)
        bias_v = r.small[s, 7:8, half_width : half_width + head_width]
        key_rows = dot_nt(normed, r.wq[s, head_width : 2 * head_width])
        value_rows = dot_nt(normed, r.wq[s, 2 * head_width : 3 * head_width]) + bias_v
        r.kv[s, 0, place] = key_rows.astype(LOW)
        r.kv[s, 1, place] = value_rows.astype(LOW)
        gather_sent(r.nrm, s, 0, j)

    def ask(s, j):
        queries = dot_nt(r.nrm[s, j], r.wq[s, 0:head_width]) + r.small[s, 7:8, :head_width]
        r.qry[s, j] = queries.astype(LOW)

    def attend_line(s, j):
        mixed = []
        for head in range(heads):
            cols = head_cols(head)
            times = multiplicity(s, j, head)
            scores = scale * dot_nt(r.qry[s, j, :, cols], r.kv[s, 0, :, cols])
            scores = jnp.where(times > 0.0, scores, MASKED)
            top = jnp.max(scores, axis=-1, keepdims=True)
            terms = times * jnp.exp(scores - top)
            weights = terms / jnp.sum(terms, axis=-1, keepdims=True)
            r.soft[s, j, head] = weights
            mixed.append(dot_nn(weights.astype(LOW), r.kv[s, 1, :, cols]))
        r.mix[s, j] = (jnp.concatenate(mixed, axis=-1) * stream_mask(j)).astype(LOW)

    def leave_attention(s, j):
        scatter_start(s, 0, j, dot_nn(r.mix[s, j], r.wo[s]))

    @on_owner
    def between(s, j):
        middle = r.hidden[j] + scatter_sum(s, 0, j) + r.small[s, 4:5]
        r.middle[j] = middle
        xhat, inverse = standard(middle)
        r.xhat2[s, j] = xhat
        r.inv2[s, j] = jnp.broadcast_to(inverse, (owned, 128))
        r.nmlp[s, j, mine] = (xhat * r.small[s, 2:3] + r.small[s, 3:4]).astype(LOW)
        gather_start(r.nmlp, s, 1, j)

    def feed(s, j):
        gather_wait(r.nmlp, s, 1, j)
        before = dot_nn(r.nmlp[s, j], r.wf[s]) + r.small[s, 6:7, :units]
        bend = jnp.tanh(0.7978845608028654 * (before + 0.044715 * before * before * before))
        r.act[s, j] = (0.5 * before * (1.0 + bend)).astype(LOW)
        r.slope[s, j] = 0.5 * (1.0 + bend) + 0.5 * before * (1.0 - bend * bend) * (
            0.7978845608028654 * (1.0 + 3 * 0.044715 * before * before)
        )

        gather_sent(r.nmlp, s, 1, j)

    def leave_feed(s, j):
        scatter_start(s, 1, j, dot_nn(r.act[s, j], r.wp[s]))

    @on_owner
    def finish(s, j):
        result = r.middle[j] + scatter_sum(s, 1, j) + r.small[s, 5:6]
        r.out_low[s, j] = result.astype(LOW)
        r.hidden[j] = result.astype(LOW).astype(F32)

    def small_ready(s):
        @pl.when(a != s)
        def _():
            small_copy(0, a, s).wait_recv()

    small_ready(0)
    for j in streams:
        first_rows(j)
        enter(0, j)

    def forward(s, _):
        need(s, 0)
        need(s, 1)

        @pl.when(a != s)
        def _():
            count_copy(0, a, s).wait_recv()

        for j in streams:
            project(s, j)

            @pl.when(c == 0)
            def _():
                kv_copy(s, j).start()

            ask(s, j)
            if j == 0:

                @pl.when(c == 1)
                def _():
                    for other in streams:
                        kv_copy(s, other).wait_recv()

            attend_line(s, j)
            leave_attention(s, j)

        @pl.when(s == 0)
        def _():
            pass_all(0, (2,))
            for later in range(1, lines):
                pass_all(later, (0, 1, 2))

        @pl.when(s == 1)
        def _():
            pass_far(1, 2)
            pass_far(1, 3)
            for later in range(2, lines):
                for p in range(4):
                    pass_far(later, p)

        for j in streams:
            between(s, j)
            scatter_sent(s, 0, j)
        @pl.when(s == 0)
        def _():
            for later in range(lines):
                pass_all(later, (3,))

        need(s, 2)
        for j in streams:
            feed(s, j)
            if j == 0:
                need(s, 3)
            leave_feed(s, j)


        @pl.when(s >= 2)
        def _():
            forward_rows(s - 2)


        @pl.when(s + 1 < lines)
        def _():
            small_ready(s + 1)

        for j in streams:
            finish(s, j)
            scatter_sent(s, 1, j)

            @pl.when(s + 1 < lines)
            def _():
                enter(s + 1, j)

        home_start(out_home, s)

        @pl.when(s == 0)
        def _():
            pass_far(1, 0)
            pass_far(1, 1)

        return 0

    lax.fori_loop(0, lines, forward, 0)

    @on_owner
    def turn(s, j):
        upstream = r.upstream[j]
        r.ups[s, j, mine] = upstream
        gather_start(r.ups, s, 2, j)
        r.norm_part[s, 5:6] += column_sum(upstream)

    def feed_back(s, j):
        gather_wait(r.ups, s, 2, j)
        grad_pre = (dot_nt(r.ups[s, j], r.wp[s]) * r.slope[s, j]).astype(LOW)
        r.gpre[s, j] = grad_pre
        scatter_start(s, 2, j, dot_nt(grad_pre, r.wf[s]))
        r.norm_part[s, 6:7, :units] += column_sum(grad_pre)
        gather_sent(r.ups, s, 2, j)

    @on_owner
    def between_back(s, j):
        grad = scatter_sum(s, 2, j)
        xhat = r.xhat2[s, j]
        upstream = r.upstream[j].astype(F32)
        grad_middle = upstream + standard_back(
            grad * r.small[s, 2:3], xhat, r.inv2[s, j, :, 0:1]
        )
        r.middle[j] = grad_middle
        branch = grad_middle.astype(LOW)
        r.brn[s, j, mine] = branch
        gather_start(r.brn, s, 3, j)
        r.norm_part[s, 2:3] += column_sum(grad * xhat)
        r.norm_part[s, 3:4] += column_sum(grad)
        r.norm_part[s, 4:5] += column_sum(branch)

    def mixed_back(s, j):
        gather_wait(r.brn, s, 3, j)
        r.gmix[j] = (dot_nt(r.brn[s, j], r.wo[s]) * stream_mask(j)).astype(LOW)
        gather_sent(r.brn, s, 3, j)

    def attend_line_back(s, j):
        grad_q, grad_k, grad_v = [], [], []
        for head in range(heads):
            cols = head_cols(head)
            weights = r.soft[s, j, head]
            grad_head = r.gmix[j, :, cols]
            grad_weights = dot_nt(grad_head, r.kv[s, 1, :, cols])
            inner = jnp.sum(weights * grad_weights, axis=-1, keepdims=True)
            grad_scores = (weights * (grad_weights - inner)).astype(LOW)
            grad_k.append(scale * dot_tn(grad_scores, r.qry[s, j, :, cols]))
            grad_v.append(dot_tn(weights.astype(LOW), grad_head))
            grad_q.append(scale * dot_nn(grad_scores, r.kv[s, 0, :, cols]))
        for which, grad in enumerate((grad_k, grad_v)):
            grad = jnp.concatenate(grad, axis=-1)
            r.dkv_all[which] = grad if j == STREAMS - 1 else r.dkv_all[which] + grad
        grad_q = jnp.concatenate(grad_q, axis=-1).astype(LOW)
        r.dqkv[s, 0, j] = grad_q
        r.norm_part[s, 7:8, :head_width] += column_sum(grad_q)

    def join_keys(s, j):
        for which in range(2):
            joined = r.dkv_all[which, row_block(c * STREAMS + j, stream_rows)].astype(LOW)
            r.dqkv[s, 1 + which, j] = joined
            if which == 1:
                lanes = slice(half_width, half_width + head_width)
                r.norm_part[s, 7:8, lanes] += column_sum(joined)

    def leave_back(s, j):
        product = dot_nn(r.dqkv[s, 0, j], r.wq[s, 0:head_width])
        for which in range(1, 3):
            weight = r.wq[s, which * head_width : (which + 1) * head_width]
            product = product + dot_nn(r.dqkv[s, which, j], weight)
        scatter_start(s, 3, j, product)

    @on_owner
    def finish_back(s, j):
        grad = scatter_sum(s, 3, j)
        xhat = r.xhat1[s, j]
        result = r.middle[j] + standard_back(
            grad * r.small[s, 0:1], xhat, r.inv1[s, j, :, 0:1]
        )
        r.upstream[j] = result.astype(LOW)
        r.grad_low[s, j] = result.astype(LOW)
        r.norm_part[s, 0:1] += column_sum(grad * xhat)
        r.norm_part[s, 1:2] += column_sum(grad)

    last_first = tuple(reversed(streams))
    for j in last_first:
        turn(lines - 1, j)

    def backward(index, _):
        s = lines - 1 - index
        for j in last_first:
            feed_back(s, j)
        rows_start(UPS, s)
        rows_start(GPRE, s)

        @pl.when(index < 2)
        def _():
            forward_rows(lines - 2 + index)

        @pl.when(index == lines - 1)
        def _():
            share(ACT)
            share(MIX)

        for j in last_first:
            between_back(s, j)
            scatter_sent(s, 2, j)
        for j in last_first:
            mixed_back(s, j)
            attend_line_back(s, j)

            @pl.when(c == 1)
            def _():
                join_keys(s, j)
                leave_back(s, j)

        rows_start(BRN, s)

        @pl.when(c == 1)
        def _():
            r.dkv_out[s] = r.dkv_all[:, 0:local].astype(LOW)
            dkv_copy(s).start()

        @pl.when(c == 0)
        def _():
            dkv_copy(s).wait_recv()
            r.dkv_all[:, 0:local] += r.dkv_in[s].astype(F32)
            for j in last_first:
                join_keys(s, j)
                leave_back(s, j)

        rows_start(DQKV, s)
        for j in last_first:
            finish_back(s, j)
            scatter_sent(s, 3, j)

            @pl.when(s > 0)
            def _():
                turn(s - 1, j)

        norm_start(s)
        home_start(grad_home, s)
        return 0

    lax.fori_loop(0, lines, backward, 0)

    share(GPRE)
    share(DQKV)

    drain(r.norm_all, r.norm_r)
    slot = c * chips + t
    norm_sum = r.norm_all[0]
    for line in range(1, lines):
        norm_sum = norm_sum + r.norm_all[line]
    r.ends[slot] = norm_sum

    def ends_copy(step):
        core, chip = step // chips, step % chips
        view = r.ends.at[slot]
        return remote(
            view,
            view,
            r.ends_s.at[step - 1],
            r.ends_r,
            seq=(c + core) % 2,
            tensor=(t + chip) % chips,
        )

    for step in range(1, 2 * chips):
        ends_copy(step).start()

    for index in range(ACT):
        drain(all_rows[index], r.rows_r.at[index])
    for index in range(ACT, 8):
        share_copy(index, 1 - c).wait_recv()
        share_copy(index, c).wait_send()
    drain(r.acts, r.out_r)
    drain(r.grads, r.grad_r)
    drain(r.ends.at[0 : 2 * chips - 1], r.ends_r)
    for step in range(1, 2 * chips):
        ends_copy(step).wait_send()
    for step in range(1, lines):
        small_copy(step - 1, (a + step) % lines, a).wait_send()
        count_copy(step - 1, (a + step) % lines, a).wait_send()
    for p in range(4):
        for which, line in enumerate((beside(a), above(a))):
            first_hop(p, a, line, which).wait_send()

    for owner in (1, 2):

        @pl.when(t != owner)
        def _():
            first_copy(owner, t).wait_send()

    def sent(s, _):
        home_sent(out_home, s)
        home_sent(grad_home, s)

        @pl.when(a != s)
        def _():
            norm_copy(s).wait_send()

        @pl.when(c == 0)
        def _():
            for j in streams:
                kv_copy(s, j).wait_send()

        @pl.when(c == 1)
        def _():
            dkv_copy(s).wait_send()

        for index in range(8):
            rows_sent(index, s)
        for p in range(4):

            @pl.when((a == beside(s)) | (a == above(s)))
            def _():
                second_hop(p, s, 0).wait_send()

            @pl.when(a != s)
            def _():
                core_hop(p, s, c).wait_send()

        return 0

    lax.fori_loop(0, lines, sent, 0)


def relay_call(inputs, cotangent, lengths, chosen, singles, weights):
    lines = lax.axis_size("section")
    chips = lax.axis_size("tensor")
    rows, buckets, width = inputs.shape[1:]
    local, total, half = rows * chips, 2 * rows * chips, width // 2
    head_width, units = weights["wo_in"].shape[0], weights["wp_in"].shape[0]
    heads = head_width // HDIM
    stream = local // STREAMS
    peers, owned = chips - 1, stream // 2
    vmem, dma = pltpu.VMEM, pltpu.SemaphoreType.DMA
    operands = dict(
        inputs=inputs,
        cotangent=cotangent,
        lengths=lengths,
        chosen=chosen,
        **singles,
        **weights,
    )

    def space(name):
        if name in weights:
            return pl.ANY
        return pltpu.SMEM if operands[name] is lengths else pltpu.VMEM

    sums = dict(
        acts=((lines, rows, width), LOW),
        grads=((lines, rows, width), LOW),
        ends=((2 * chips, 8, width), F32),
    )
    gathered = dict(
        all_nrm=((lines, 2, STREAMS, stream, half), LOW),
        all_nmlp=((lines, 2, STREAMS, stream, half), LOW),
        all_ups=((lines, 2, STREAMS, stream, half), LOW),
        all_brn=((lines, 2, STREAMS, stream, half), LOW),
        all_act=((lines, 2, STREAMS, stream, units), LOW),
        all_gpre=((lines, 2, STREAMS, stream, units), LOW),
        all_mix=((lines, 2, STREAMS, stream, head_width), LOW),
        all_dqkv=((lines, 2, 3, STREAMS, stream, head_width), LOW),
    )
    outputs = dict(**sums, **gathered)
    scratch = dict(
        wq=vmem((lines,) + weights["wq_in"].shape, LOW),
        wo=vmem((lines,) + weights["wo_in"].shape, LOW),
        wf=vmem((lines,) + weights["wf_in"].shape, LOW),
        wp=vmem((lines,) + weights["wp_in"].shape, LOW),
        small_own=vmem((8, width), F32),
        small=vmem((lines, 8, width), F32),
        count_own=vmem((lines, 8, total), F32),
        count=vmem((lines, 8, total), F32),
        hidden=vmem((STREAMS, owned, width), F32),
        middle=vmem((STREAMS, owned, width), F32),
        upstream=vmem((STREAMS, owned, width), LOW),
        first_out=vmem((2, 2, owned, width), LOW),
        first_in=vmem((STREAMS, 2, owned, width), LOW),
        xhat1=vmem((lines, STREAMS, owned, width), F32),
        inv1=vmem((lines, STREAMS, owned, 128), F32),
        xhat2=vmem((lines, STREAMS, owned, width), F32),
        inv2=vmem((lines, STREAMS, owned, 128), F32),
        nrm=vmem((lines, STREAMS, stream, width), LOW),
        nmlp=vmem((lines, STREAMS, stream, width), LOW),
        ups=vmem((lines, STREAMS, stream, width), LOW),
        brn=vmem((lines, STREAMS, stream, width), LOW),
        act=vmem((lines, STREAMS, stream, units), LOW),
        gpre=vmem((lines, STREAMS, stream, units), LOW),
        slope=vmem((lines, STREAMS, stream, units), F32),
        mix=vmem((lines, STREAMS, stream, head_width), LOW),
        qry=vmem((lines, STREAMS, stream, head_width), LOW),
        gmix=vmem((STREAMS, stream, head_width), LOW),
        dqkv=vmem((lines, 3, STREAMS, stream, head_width), LOW),
        kv=vmem((lines, 2, total, head_width), LOW),
        soft=vmem((lines, STREAMS, heads, stream, total), F32),
        near=vmem((STREAMS, stream, total), F32),
        dkv_all=vmem((2, total, head_width), F32),
        dkv_out=vmem((lines, 2, local, head_width), LOW),
        dkv_in=vmem((lines, 2, local, head_width), LOW),
        part=vmem((4, STREAMS, stream, width), LOW),
        arrived=vmem((lines, 4, STREAMS, peers, owned, width), LOW),
        out_low=vmem((lines, STREAMS, owned, width), LOW),
        grad_low=vmem((lines, STREAMS, owned, width), LOW),
        norm_part=vmem((lines, 8, width), F32),
        norm_all=vmem((lines, 8, width), F32),
        w_first_s=dma((4, 2)),
        w_first_r=dma((lines, 4)),
        w_second_s=dma((lines, 4)),
        w_second_r=dma((lines, 4, 2)),
        w_core_s=dma((lines, 4)),
        w_core_r=dma((lines, 4)),
        w_own=dma((4,)),
        small_s=dma((lines - 1,)),
        small_r=dma((lines,)),
        count_s=dma((lines - 1,)),
        count_r=dma((lines,)),
        ag_s=dma((4, STREAMS, peers)),
        ag_r=dma((4, STREAMS, peers)),
        rs_s=dma((4, STREAMS, peers)),
        rs_r=dma((4, STREAMS, peers)),
        kv_s=dma((lines, STREAMS)),
        kv_r=dma((lines, STREAMS)),
        dkv_s=dma((lines,)),
        dkv_r=dma((lines,)),
        rows_s=dma((8, lines, 2)),
        rows_r=dma((8,)),
        share_s=dma((4,)),
        share_r=dma((4,)),
        first_s=dma((2,)),
        first_r=dma((STREAMS,)),
        out_s=dma((lines, STREAMS)),
        out_r=dma,
        grad_s=dma((lines, STREAMS)),
        grad_r=dma,
        norm_s=dma((lines,)),
        norm_r=dma,
        ends_s=dma((2 * chips - 1,)),
        ends_r=dma,
    )
    names = tuple(operands) + tuple(outputs) + tuple(scratch)
    results = pl.pallas_call(
        functools.partial(relay_kernel, names),
        out_shape=[jax.ShapeDtypeStruct(shape, kind) for shape, kind in outputs.values()],
        in_specs=[pl.BlockSpec(memory_space=space(name)) for name in operands],
        out_specs=[
            pl.BlockSpec(memory_space=pl.ANY if name in gathered else pltpu.VMEM)
            for name in outputs
        ],
        scratch_shapes=list(scratch.values()),
        compiler_params=pltpu.CompilerParams(
            collective_id=0, has_side_effects=True, vmem_limit_bytes=60 * 2**20
        ),
        name="relay",
    )(*operands.values())
    return dict(zip(outputs, results))


def weights_kernel(names, *refs):
    r = types.SimpleNamespace(**dict(zip(names, refs)))
    step = pl.program_id(0)
    micro_count, rows, buckets, width = r.activations.shape
    chips, units, head_width = r.ends.shape[0] // 2, r.all_act.shape[-1], r.all_mix.shape[-1]

    @pl.when(step == 0)
    def _():
        sums = r.ends[0]
        for other in range(1, 2 * chips):
            sums = sums + r.ends[other]
        singles = (r.ln1_gain, r.ln1_shift, r.ln2_gain, r.ln2_shift, r.b_out, r.b_proj)
        for place, single in enumerate(singles):
            single[...] = sums[place : place + 1]
        for chip in range(chips):
            both = r.ends[chip] + r.ends[chips + chip]
            r.b_fc[:, chip * units : (chip + 1) * units] = both[6:7, :units]
            here = slice(chip * head_width, (chip + 1) * head_width)
            r.b_qv[0:1, here] = both[7:8, :head_width]
            r.b_qv[1:2, here] = both[7:8, width // 2 : width // 2 + head_width]
        for target, source in ((r.activations, r.acts), (r.in_grads, r.grads)):
            for micro in range(micro_count):
                rows_of = [
                    source[micro * buckets + bucket].astype(F32)[:, None, :]
                    for bucket in range(buckets)
                ]
                target[micro] = jnp.concatenate(rows_of, axis=1).astype(LOW)
        for target in (r.w_qkv, r.w_out, r.w_fc, r.w_proj):
            target[...] = jnp.zeros_like(target)

    def rows_of_sequence(ref):
        return ref[0].reshape(2 * chips * rows, ref.shape[-1])

    nrm, nmlp, ups, brn, act, gpre, mix = (
        rows_of_sequence(ref)
        for ref in (r.all_nrm, r.all_nmlp, r.all_ups, r.all_brn, r.all_act, r.all_gpre, r.all_mix)
    )
    r.w_proj[...] += dot_tn(act, ups)
    r.w_fc[...] += dot_tn(nmlp, gpre)
    r.w_out[...] += dot_tn(mix, brn)
    for which in range(3):
        grad = r.all_dqkv[0, :, which].reshape(2 * chips * rows, head_width)
        r.w_qkv[which] += dot_tn(grad, nrm)


def weights_call(relayed, inputs_shape, head_width, units):
    lines = lax.axis_size("section")
    chips = lax.axis_size("tensor")
    width = inputs_shape[-1]
    half = width // 2
    outputs = dict(
        activations=(inputs_shape, LOW),
        in_grads=(inputs_shape, LOW),
        ln1_gain=((1, width), F32),
        ln1_shift=((1, width), F32),
        w_qkv=((3, head_width, half), F32),
        b_qv=((2, width), F32),
        w_out=((head_width, half), F32),
        b_out=((1, width), F32),
        ln2_gain=((1, width), F32),
        ln2_shift=((1, width), F32),
        w_fc=((half, units), F32),
        b_fc=((1, chips * units), F32),
        w_proj=((units, half), F32),
        b_proj=((1, width), F32),
    )

    def spec(array):
        if len(array.shape) < 5:
            return pl.BlockSpec(array.shape, lambda step: (0,) * len(array.shape))
        return pl.BlockSpec(
            (1,) + array.shape[1:], lambda step: (step,) + (0,) * (len(array.shape) - 1)
        )

    def whole(shape):
        return pl.BlockSpec(shape, lambda step: (0,) * len(shape))

    return pl.pallas_call(
        functools.partial(weights_kernel, tuple(relayed) + tuple(outputs)),
        out_shape=[jax.ShapeDtypeStruct(shape, kind) for shape, kind in outputs.values()],
        grid=(lines,),
        in_specs=[spec(array) for array in relayed.values()],
        out_specs=[whole(shape) for shape, _ in outputs.values()],
        compiler_params=pltpu.CompilerParams(vmem_limit_bytes=60 * 2**20),
        name="weight_gradients",
    )(*relayed.values())


def on_line(
    inputs,
    cotangent,
    lengths,
    chosen,
    ln1_gain,
    ln1_shift,
    w_qkv,
    b_qv,
    w_out,
    b_out,
    ln2_gain,
    ln2_shift,
    w_fc,
    b_fc,
    w_proj,
    b_proj,
):
    head_width, units = w_out.shape[1], w_fc.shape[2]
    singles = dict(
        ln1_gain=ln1_gain,
        ln1_shift=ln1_shift,
        ln2_gain=ln2_gain,
        ln2_shift=ln2_shift,
        b_out=b_out,
        b_proj=b_proj,
        b_fc=b_fc,
        b_qv=b_qv[0],
    )
    weights = dict(
        wq_in=jnp.swapaxes(w_qkv[0], 1, 2).reshape(-1, inputs.shape[-1]),
        wo_in=w_out[0],
        wf_in=w_fc[0],
        wp_in=w_proj[0],
    )
    picks = chosen.reshape((-1,) + chosen.shape[-2:])
    relayed = relay_call(inputs, cotangent, lengths, picks, singles, weights)
    results = list(weights_call(relayed, inputs.shape, head_width, units))
    results[4] = jnp.swapaxes(results[4], 1, 2)
    vectors = (2, 3, 7, 8, 9, 11, 13)
    return tuple(
        result if place in vectors else result[None] for place, result in enumerate(results)
    )


def fits_lines(mesh):
    return mesh.shape["section"] == 4 and mesh.shape["seq"] == 2 and mesh.shape["tensor"] == 4


def solution(mesh):
    placed = (
        P(None, ("seq", "tensor"), None, None),
        P(None, ("seq", "tensor"), None, None),
        P(),
        P("section", None, None, "tensor", "seq", None),
        P("section", None),
        P("section", None),
        P("section", None, None, "tensor"),
        P("section", None, "tensor"),
        P("section", "tensor", None),
        P("section", None),
        P("section", None),
        P("section", None),
        P("section", None, "tensor"),
        P("section", "tensor"),
        P("section", "tensor", None),
        P("section", None),
    )
    return jax.shard_map(
        on_line if fits_lines(mesh) else on_device,
        mesh=mesh,
        in_specs=placed,
        out_specs=(
            P("section", None, ("seq", "tensor"), None, None),
            P("section", None, ("seq", "tensor"), None, None),
            P("section", None),
            P("section", None),
            P("section", None, "seq", "tensor"),
            P("section", None, None),
            P("section", "tensor", "seq"),
            P("section", None),
            P("section", None),
            P("section", None),
            P("section", "seq", "tensor"),
            P("section", None),
            P("section", "tensor", "seq"),
            P("section", None),
        ),
        check_vma=False,
    )
```

```python
import functools
import types

import jax
import jax.numpy as jnp
from jax import lax
from jax.experimental import pallas as pl
from jax.experimental.pallas import tpu as pltpu
from jax.sharding import PartitionSpec as P

HDIM = 64
WIN = 64
QB = 64
KSEL = 64


NORM_EPS = 1e-05
MASKED = -1000000000.0


def from_behind(value, axis, steps):
    count = lax.axis_size(axis)
    first, last = (max(0, -steps), min(count, count - steps))
    return lax.ppermute(value, axis, [(source, source + steps) for source in range(first, last)])


def layer_norm(values, gain, shift):
    average = jnp.mean(values, axis=-1, keepdims=True)
    centred = values - average
    variance = jnp.mean(centred * centred, axis=-1, keepdims=True)
    return centred * lax.rsqrt(variance + NORM_EPS) * gain + shift


def gelu_tanh(values):
    return (
        0.5
        * values
        * (1.0 + jnp.tanh(0.7978845608028654 * (values + 0.044715 * values * values * values)))
    )


def gather_rows(row_block):
    return lax.all_gather(row_block, "tensor", axis=0, tiled=True)


def scatter_product(left_rows, weight, formula):
    return lax.psum_scatter(
        jnp.einsum(formula, left_rows, weight, preferred_element_type=jnp.float32).astype(
            jnp.bfloat16
        ),
        "tensor",
        scatter_dimension=0,
        tiled=True,
    ).astype(jnp.float32)


def near_slabs(full_rows, seq_start, seq_first, length_local):
    buckets = full_rows.shape[1]
    heads_local = full_rows.shape[2] // HDIM
    blocks = length_local // QB
    earlier = lax.dynamic_slice_in_dim(full_rows, jnp.maximum(seq_start - WIN, 0), WIN, 0)
    earlier = jnp.where(seq_first, jnp.zeros_like(earlier), earlier)
    local_part = lax.dynamic_slice_in_dim(full_rows, seq_start, length_local, 0)
    segment = jnp.concatenate([earlier, local_part], 0).reshape(
        length_local + WIN, buckets, heads_local, HDIM
    )
    return jnp.concatenate(
        [
            segment[offset_index * QB : offset_index * QB + length_local].reshape(
                blocks, QB, buckets, heads_local, HDIM
            )
            for offset_index in range(WIN // QB + 1)
        ],
        1,
    )


def far_rows(full_rows, flat_index):
    total_rows, buckets, feature_width = full_rows.shape
    heads_local = feature_width // HDIM
    return jnp.take(full_rows.reshape(total_rows * buckets * heads_local, HDIM), flat_index, axis=0)


def key_geometry(chosen_now, seq_start, blocks):
    buckets, heads_local = (chosen_now.shape[0], chosen_now.shape[1])
    bucket_ids = lax.broadcasted_iota(jnp.int32, chosen_now.shape, 0)
    head_ids = lax.broadcasted_iota(jnp.int32, chosen_now.shape, 1)
    flat_index = (chosen_now * buckets + bucket_ids) * heads_local + head_ids
    block_start = seq_start + QB * lax.broadcasted_iota(jnp.int32, (blocks, 1, 1), 0)
    query_ids = lax.broadcasted_iota(jnp.int32, (1, QB, 1), 1)
    key_ids = lax.broadcasted_iota(jnp.int32, (1, 1, WIN + QB), 2)
    distance = query_ids + WIN - key_ids
    near_ok = (distance >= 0) & (distance < WIN) & (block_start + key_ids - WIN >= 0)
    far_ok = chosen_now + WIN <= block_start.reshape(1, 1, blocks, 1)
    near_mask = jnp.broadcast_to(
        near_ok[:, None, None], (blocks, buckets, heads_local, QB, WIN + QB)
    )
    far_mask = jnp.broadcast_to(
        jnp.transpose(far_ok, (2, 0, 1, 3))[:, :, :, None, :],
        (blocks, buckets, heads_local, QB, KSEL),
    )
    return (flat_index, jnp.concatenate([near_mask, far_mask], -1))


def attention_setup(queries, key_rows, value_rows, chosen_now, seq_start, seq_first):
    length_local, buckets, feature_width = queries.shape
    heads_local = feature_width // HDIM
    blocks = length_local // QB
    query_blocks = queries.reshape(blocks, QB, buckets, heads_local, HDIM)
    flat_index, key_mask = key_geometry(chosen_now, seq_start, blocks)
    near_keys = near_slabs(key_rows, seq_start, seq_first, length_local)
    near_values = near_slabs(value_rows, seq_start, seq_first, length_local)
    far_keys = far_rows(key_rows, flat_index)
    far_values = far_rows(value_rows, flat_index)
    near_scores = jnp.einsum(
        "bqnhe,btnhe->bnhqt", query_blocks, near_keys, preferred_element_type=jnp.float32
    )
    far_scores = jnp.einsum(
        "bqnhe,nhbke->bnhqk", query_blocks, far_keys, preferred_element_type=jnp.float32
    )
    scores = jnp.where(
        key_mask, HDIM ** (-0.5) * jnp.concatenate([near_scores, far_scores], -1), MASKED
    )
    return (query_blocks, near_keys, near_values, far_keys, far_values, flat_index, scores)


def attend(queries, key_rows, value_rows, chosen_now, seq_start, seq_first):
    query_blocks, near_keys, near_values, far_keys, far_values, flat_index, scores = (
        attention_setup(queries, key_rows, value_rows, chosen_now, seq_start, seq_first)
    )
    span = WIN + QB
    row_top = jnp.max(scores, -1, keepdims=True)
    exp_terms = jnp.exp(scores - row_top)
    row_total = jnp.sum(exp_terms, -1, keepdims=True)
    softmax_low = (exp_terms / row_total).astype(jnp.bfloat16)
    near_part = jnp.einsum(
        "bnhqt,btnhe->bqnhe",
        softmax_low[..., :span],
        near_values,
        preferred_element_type=jnp.float32,
    )
    far_part = jnp.einsum(
        "bnhqk,nhbke->bqnhe",
        softmax_low[..., span:],
        far_values,
        preferred_element_type=jnp.float32,
    )
    return ((near_part + far_part).reshape(queries.shape), row_top + jnp.log(row_total))


def spread_back(near_grad, far_grad, flat_index, seq_start, seq_first, total_rows):
    blocks, span, buckets, heads_local, head_size = near_grad.shape
    length_local = blocks * QB
    feature_width = heads_local * head_size
    segment = jnp.zeros((length_local + WIN, buckets, heads_local, head_size), jnp.float32)
    for offset_index in range(WIN // QB + 1):
        piece = near_grad[:, offset_index * QB : (offset_index + 1) * QB].reshape(
            length_local, buckets, heads_local, head_size
        )
        segment = segment.at[offset_index * QB : offset_index * QB + length_local].add(piece)
    full_rows = jnp.zeros((total_rows * buckets * heads_local, head_size), jnp.float32)
    full_rows = full_rows.at[flat_index.reshape(-1)].add(far_grad.reshape(-1, head_size))
    full_rows = full_rows.reshape(total_rows, buckets, feature_width)
    local_part = segment[WIN:].reshape(length_local, buckets, feature_width)
    earlier = jnp.where(seq_first, 0.0, segment[:WIN].reshape(WIN, buckets, feature_width))
    full_rows = lax.dynamic_update_slice_in_dim(
        full_rows,
        lax.dynamic_slice_in_dim(full_rows, seq_start, length_local, 0) + local_part,
        seq_start,
        0,
    )
    earlier_start = jnp.maximum(seq_start - WIN, 0)
    full_rows = lax.dynamic_update_slice_in_dim(
        full_rows,
        lax.dynamic_slice_in_dim(full_rows, earlier_start, WIN, 0) + earlier,
        earlier_start,
        0,
    )
    return full_rows


def attend_back(
    queries, key_rows, value_rows, chosen_now, seq_start, seq_first, log_total, grad_mixed
):
    query_blocks, near_keys, near_values, far_keys, far_values, flat_index, scores = (
        attention_setup(queries, key_rows, value_rows, chosen_now, seq_start, seq_first)
    )
    span = WIN + QB
    score_scale = HDIM ** (-0.5)
    grad_blocks = grad_mixed.reshape(query_blocks.shape)
    weights_full = jnp.exp(scores - log_total)
    softmax_low = weights_full.astype(jnp.bfloat16)
    grad_near_weights = jnp.einsum(
        "bqnhe,btnhe->bnhqt", grad_blocks, near_values, preferred_element_type=jnp.float32
    )
    grad_far_weights = jnp.einsum(
        "bqnhe,nhbke->bnhqk", grad_blocks, far_values, preferred_element_type=jnp.float32
    )
    grad_weights = jnp.concatenate([grad_near_weights, grad_far_weights], -1)
    row_dot = jnp.sum(weights_full * grad_weights, -1, keepdims=True)
    grad_scores = (weights_full * (grad_weights - row_dot)).astype(jnp.bfloat16)
    grad_near, grad_far = (grad_scores[..., :span], grad_scores[..., span:])
    grad_queries = score_scale * (
        jnp.einsum("bnhqt,btnhe->bqnhe", grad_near, near_keys, preferred_element_type=jnp.float32)
        + jnp.einsum("bnhqk,nhbke->bqnhe", grad_far, far_keys, preferred_element_type=jnp.float32)
    )
    near_key_grad = score_scale * jnp.einsum(
        "bnhqt,bqnhe->btnhe", grad_near, query_blocks, preferred_element_type=jnp.float32
    )
    far_key_grad = score_scale * jnp.einsum(
        "bnhqk,bqnhe->nhbke", grad_far, query_blocks, preferred_element_type=jnp.float32
    )
    near_value_grad = jnp.einsum(
        "bnhqt,bqnhe->btnhe",
        softmax_low[..., :span],
        grad_blocks,
        preferred_element_type=jnp.float32,
    )
    far_value_grad = jnp.einsum(
        "bnhqk,bqnhe->nhbke",
        softmax_low[..., span:],
        grad_blocks,
        preferred_element_type=jnp.float32,
    )
    total_rows = key_rows.shape[0]
    key_grad = spread_back(
        near_key_grad, far_key_grad, flat_index, seq_start, seq_first, total_rows
    )
    value_grad = spread_back(
        near_value_grad, far_value_grad, flat_index, seq_start, seq_first, total_rows
    )
    return (grad_queries.reshape(queries.shape), key_grad, value_grad)


def forward_pass(hidden, params, chosen_now, query_mask, seq_start, seq_first, finish):
    (
        ln1_gain,
        ln1_shift,
        w_qkv,
        b_qv,
        w_out,
        b_out,
        ln2_gain,
        ln2_shift,
        w_fc,
        b_fc,
        w_proj,
        b_proj,
    ) = params
    hidden_wide = hidden.astype(jnp.float32)
    normed_all = gather_rows(layer_norm(hidden_wide, ln1_gain, ln1_shift).astype(jnp.bfloat16))
    projected = jnp.einsum("pnd,jdc->jpnc", normed_all, w_qkv, preferred_element_type=jnp.float32)
    queries = (projected[0] + b_qv[0]).astype(jnp.bfloat16)
    key_rows, value_rows = (
        lax.all_gather(projected[1].astype(jnp.bfloat16), "seq", axis=0, tiled=True),
        lax.all_gather((projected[2] + b_qv[1]).astype(jnp.bfloat16), "seq", axis=0, tiled=True),
    )
    attended, log_total = attend(queries, key_rows, value_rows, chosen_now, seq_start, seq_first)
    mixed_rows = (attended * query_mask[:, :, None]).astype(jnp.bfloat16)
    middle = hidden_wide + scatter_product(mixed_rows, w_out, "pnc,cd->pnd") + b_out
    normed_mlp = gather_rows(layer_norm(middle, ln2_gain, ln2_shift).astype(jnp.bfloat16))
    pre_active = (
        jnp.einsum("pnd,df->pnf", normed_mlp, w_fc, preferred_element_type=jnp.float32) + b_fc
    )
    active = gelu_tanh(pre_active).astype(jnp.bfloat16)
    if not finish:
        return (
            normed_all,
            queries,
            key_rows,
            value_rows,
            log_total,
            mixed_rows,
            middle,
            normed_mlp,
            pre_active,
            active,
        )
    output = (middle + scatter_product(active, w_proj, "pnf,fd->pnd") + b_proj).astype(jnp.bfloat16)
    return (output, (key_rows, value_rows))


def backward_pass(hidden, upstream, params, chosen_now, query_mask, seq_start, seq_first):
    (
        ln1_gain,
        ln1_shift,
        w_qkv,
        b_qv,
        w_out,
        b_out,
        ln2_gain,
        ln2_shift,
        w_fc,
        b_fc,
        w_proj,
        b_proj,
    ) = params
    (
        normed_all,
        queries,
        key_rows,
        value_rows,
        log_total,
        mixed_rows,
        middle,
        normed_mlp,
        pre_active,
        active,
    ) = forward_pass(hidden, params, chosen_now, query_mask, seq_start, seq_first, False)
    upstream_all = gather_rows(upstream)
    grad_w_proj = jnp.einsum(
        "pnf,pnd->fd", active, upstream_all, preferred_element_type=jnp.float32
    )
    grad_b_proj = jnp.sum(upstream.astype(jnp.float32), axis=(0, 1))
    grad_active = jnp.einsum(
        "pnd,fd->pnf", upstream_all, w_proj, preferred_element_type=jnp.float32
    )
    unused_value, gelu_pull = jax.vjp(gelu_tanh, pre_active)
    grad_pre = gelu_pull(grad_active)[0].astype(jnp.bfloat16)
    grad_w_fc = jnp.einsum("pnd,pnf->df", normed_mlp, grad_pre, preferred_element_type=jnp.float32)
    grad_b_fc = jnp.sum(grad_pre.astype(jnp.float32), axis=(0, 1))
    grad_normed_mlp = scatter_product(grad_pre, w_fc, "pnf,df->pnd")
    unused_norm, second_pull = jax.vjp(layer_norm, middle, ln2_gain, ln2_shift)
    grad_mid_norm, grad_ln2_gain, grad_ln2_shift = second_pull(grad_normed_mlp)
    grad_middle = upstream.astype(jnp.float32) + grad_mid_norm
    grad_branch = grad_middle.astype(jnp.bfloat16)
    grad_b_out = jnp.sum(grad_branch.astype(jnp.float32), axis=(0, 1))
    branch_all = gather_rows(grad_branch)
    grad_w_out = jnp.einsum(
        "pnc,pnd->cd", mixed_rows, branch_all, preferred_element_type=jnp.float32
    )
    grad_mixed = jnp.einsum(
        "pnd,cd->pnc", branch_all, w_out, preferred_element_type=jnp.float32
    ).astype(jnp.bfloat16) * query_mask[:, :, None].astype(jnp.bfloat16)
    grad_queries, key_grad_all, value_grad_all = attend_back(
        queries, key_rows, value_rows, chosen_now, seq_start, seq_first, log_total, grad_mixed
    )
    key_grad, value_grad = (
        lax.psum_scatter(
            key_grad_all.astype(jnp.bfloat16), "seq", scatter_dimension=0, tiled=True
        ).astype(jnp.float32),
        lax.psum_scatter(
            value_grad_all.astype(jnp.bfloat16), "seq", scatter_dimension=0, tiled=True
        ).astype(jnp.float32),
    )
    grad_project = jnp.stack(
        [
            grad_queries.astype(jnp.bfloat16),
            key_grad.astype(jnp.bfloat16),
            value_grad.astype(jnp.bfloat16),
        ],
        2,
    )
    grad_w_qkv = jnp.einsum(
        "pnd,pnjc->jdc", normed_all, grad_project, preferred_element_type=jnp.float32
    )
    grad_b_qv = jnp.sum(grad_project[:, :, 0::2].astype(jnp.float32), axis=(0, 1))
    grad_normed = scatter_product(grad_project, w_qkv, "pnjc,jdc->pnd")
    unused_first, first_pull = jax.vjp(layer_norm, hidden.astype(jnp.float32), ln1_gain, ln1_shift)
    grad_in_norm, grad_ln1_gain, grad_ln1_shift = first_pull(grad_normed)
    grad_hidden = (grad_middle + grad_in_norm).astype(jnp.bfloat16)
    block_grads = (
        grad_ln1_gain,
        grad_ln1_shift,
        grad_w_qkv,
        grad_b_qv,
        grad_w_out,
        grad_b_out,
        grad_ln2_gain,
        grad_ln2_shift,
        grad_w_fc,
        grad_b_fc,
        grad_w_proj,
        grad_b_proj,
    )
    return (grad_hidden, block_grads)


def on_device(
    inputs,
    cotangent,
    lengths,
    chosen,
    ln1_gain,
    ln1_shift,
    w_qkv,
    b_qv,
    w_out,
    b_out,
    ln2_gain,
    ln2_shift,
    w_fc,
    b_fc,
    w_proj,
    b_proj,
):
    params = tuple(
        (
            weight_array[0]
            for weight_array in (
                ln1_gain,
                ln1_shift,
                w_qkv,
                b_qv,
                w_out,
                b_out,
                ln2_gain,
                ln2_shift,
                w_fc,
                b_fc,
                w_proj,
                b_proj,
            )
        )
    )
    section_index = lax.axis_index("section")
    section_count = lax.axis_size("section")
    seq_index = lax.axis_index("seq")
    tensor_index = lax.axis_index("tensor")
    tensor_count = lax.axis_size("tensor")
    micro_count, rows_local, buckets, feature_width = inputs.shape
    length_local = rows_local * tensor_count
    heads_width = w_qkv.shape[-1]
    seq_start = seq_index * length_local
    seq_first = seq_index == 0
    positions = seq_start + lax.broadcasted_iota(jnp.int32, (micro_count, length_local, buckets), 1)
    mask_all = (positions < lengths[:, None, :]).astype(jnp.float32)
    mask_rows = lax.dynamic_slice_in_dim(mask_all, tensor_index * rows_local, rows_local, 1)
    step_count = micro_count + section_count - 1
    chosen_section = chosen[0]
    received = jnp.zeros((rows_local, buckets, feature_width), jnp.bfloat16)
    stored = jnp.zeros((micro_count, rows_local, buckets, feature_width), jnp.bfloat16)
    outputs = jnp.zeros_like(stored)
    for step_index in range(step_count):
        micro_index = step_index - section_index
        running = (micro_index >= 0) & (micro_index < micro_count)
        slot_index = jnp.clip(micro_index, 0, micro_count - 1)
        block_in = jnp.where(
            section_index == 0, lax.dynamic_index_in_dim(inputs, slot_index, 0, False), received
        )
        chosen_now = lax.dynamic_index_in_dim(chosen_section, slot_index, 0, False)
        query_mask = lax.dynamic_index_in_dim(mask_all, slot_index, 0, False)
        result, key_pair = forward_pass(
            block_in, params, chosen_now, query_mask, seq_start, seq_first, True
        )
        stored = jnp.where(
            running, lax.dynamic_update_index_in_dim(stored, block_in, slot_index, 0), stored
        )
        outputs = jnp.where(
            running, lax.dynamic_update_index_in_dim(outputs, result, slot_index, 0), outputs
        )
        received = from_behind(result, "section", 1)
    back_received = jnp.zeros((rows_local, buckets, feature_width), jnp.bfloat16)
    in_grads = jnp.zeros_like(stored)
    totals = None
    for step_index in range(step_count):
        micro_index = step_index - (section_count - 1 - section_index)
        running = (micro_index >= 0) & (micro_index < micro_count)
        slot_index = jnp.clip(micro_index, 0, micro_count - 1)
        chosen_now = lax.dynamic_index_in_dim(chosen_section, slot_index, 0, False)
        query_mask = lax.dynamic_index_in_dim(mask_all, slot_index, 0, False)
        local_mask = lax.dynamic_index_in_dim(mask_rows, slot_index, 0, False)
        top_grad = (
            lax.dynamic_index_in_dim(cotangent, slot_index, 0, False).astype(jnp.float32)
            * local_mask[:, :, None]
        ).astype(jnp.bfloat16)
        upstream = jnp.where(section_index == section_count - 1, top_grad, back_received)
        hidden = lax.dynamic_index_in_dim(stored, slot_index, 0, False)
        grad_hidden, block_grads = backward_pass(
            hidden, upstream, params, chosen_now, query_mask, seq_start, seq_first
        )
        block_grads = tuple(
            (jnp.where(running, grad_part, jnp.zeros_like(grad_part)) for grad_part in block_grads)
        )
        totals = (
            block_grads
            if step_index == 0
            else tuple(
                (total_part + grad_part for total_part, grad_part in zip(totals, block_grads))
            )
        )
        in_grads = jnp.where(
            running, lax.dynamic_update_index_in_dim(in_grads, grad_hidden, slot_index, 0), in_grads
        )
        back_received = from_behind(grad_hidden, "section", -1)
    (
        sum_ln1_gain,
        sum_ln1_shift,
        sum_w_qkv,
        sum_b_qv,
        sum_w_out,
        sum_b_out,
        sum_ln2_gain,
        sum_ln2_shift,
        sum_w_fc,
        sum_b_fc,
        sum_w_proj,
        sum_b_proj,
    ) = totals
    part_qkv, part_out, part_fc, part_proj = (
        lax.psum_scatter(
            sum_w_qkv.astype(jnp.bfloat16), "seq", scatter_dimension=1, tiled=True
        ).astype(jnp.float32),
        lax.psum_scatter(
            sum_w_out.astype(jnp.bfloat16), "seq", scatter_dimension=1, tiled=True
        ).astype(jnp.float32),
        lax.psum_scatter(
            sum_w_fc.astype(jnp.bfloat16), "seq", scatter_dimension=0, tiled=True
        ).astype(jnp.float32),
        lax.psum_scatter(
            sum_w_proj.astype(jnp.bfloat16), "seq", scatter_dimension=1, tiled=True
        ).astype(jnp.float32),
    )
    bias_qv = lax.dynamic_update_slice_in_dim(
        jnp.zeros((2, feature_width), jnp.float32), sum_b_qv, tensor_index * heads_width, 1
    )
    units_local = sum_b_fc.shape[0]
    bias_fc = lax.dynamic_update_slice_in_dim(
        jnp.zeros((units_local * tensor_count,), jnp.float32),
        sum_b_fc,
        tensor_index * units_local,
        0,
    )
    small_sums = lax.psum(
        (
            sum_ln1_gain,
            sum_ln1_shift,
            bias_qv,
            sum_b_out,
            sum_ln2_gain,
            sum_ln2_shift,
            bias_fc,
            sum_b_proj,
        ),
        ("seq", "tensor"),
    )
    return (
        outputs[None],
        in_grads[None],
        small_sums[0][None],
        small_sums[1][None],
        part_qkv[None],
        small_sums[2][None],
        part_out[None],
        small_sums[3][None],
        small_sums[4][None],
        small_sums[5][None],
        part_fc[None],
        small_sums[6][None],
        part_proj[None],
        small_sums[7][None],
    )


STREAMS = 4
NRM, NMLP, UPS, BRN, ACT, GPRE, MIX, DQKV = range(8)
F32 = jnp.float32
LOW = jnp.bfloat16
MESH_ID = pl.DeviceIdType.MESH


def dot_nn(left, right):
    return lax.dot_general(left, right, (((1,), (0,)), ((), ())), preferred_element_type=F32)


def dot_nt(left, right):
    return lax.dot_general(left, right, (((1,), (1,)), ((), ())), preferred_element_type=F32)


def dot_tn(left, right):
    return lax.dot_general(left, right, (((0,), (0,)), ((), ())), preferred_element_type=F32)


def standard(rows):
    centred = rows - jnp.mean(rows, axis=-1, keepdims=True)
    scale = lax.rsqrt(jnp.mean(centred * centred, axis=-1, keepdims=True) + NORM_EPS)
    return centred * scale, scale


def standard_back(grad, xhat, scale):
    inner = jnp.mean(grad * xhat, axis=-1, keepdims=True)
    return scale * (grad - jnp.mean(grad, axis=-1, keepdims=True) - xhat * inner)


def column_sum(rows):
    return jnp.sum(rows.astype(F32), axis=0, keepdims=True)


def relay_kernel(names, *refs):
    r = types.SimpleNamespace(**dict(zip(names, refs)))
    a, c, t = (lax.axis_index(name) for name in ("section", "seq", "tensor"))
    lines = lax.axis_size("section")
    chips = lax.axis_size("tensor")
    rows, buckets, width = r.inputs.shape[1:]
    half_width = width // 2
    local = rows * chips
    total = 2 * local
    stream_rows = local // STREAMS
    head_width = r.wo_in.shape[0]
    heads = head_width // HDIM
    blocks = local // QB
    units = r.wp_in.shape[0]
    scale = HDIM ** (-0.5)
    streams = range(STREAMS)

    def remote(src, dst, send, recv, **target):
        return pltpu.make_async_remote_copy(
            src_ref=src,
            dst_ref=dst,
            send_sem=send,
            recv_sem=recv,
            device_id=target,
            device_id_type=MESH_ID,
        )

    def drain(ref, sem):
        pltpu.make_async_copy(ref, ref, sem).wait()

    def row_block(index, size):
        return pl.ds(pl.multiple_of(index * size, size), size)

    near_chip = t + 1 - 2 * (t % 2)
    over_chip = (t + 2) % 4
    across_chip = 3 - t
    middle_chip = (t == 1) | (t == 2)
    end_chip = (t == 0) | (t == 3)
    owned = stream_rows // 2
    mine = row_block(t - 1, owned)
    my_half = row_block(c, local)

    barrier = pltpu.get_barrier_semaphore()
    for core in range(2):
        for step in range(1, chips):
            there = {"tensor": (t + step) % chips, "seq": core}
            pl.semaphore_signal(barrier, inc=1, device_id=there, device_id_type=MESH_ID)
        for step in range(1, lines):
            there = {"section": (a + step) % lines, "seq": core}
            pl.semaphore_signal(barrier, inc=1, device_id=there, device_id_type=MESH_ID)
    for step in range(1, lines):
        there = {"section": (a + step) % lines, "tensor": near_chip}
        pl.semaphore_signal(barrier, inc=1, device_id=there, device_id_type=MESH_ID)
    pl.semaphore_signal(barrier, inc=1, device_id={"seq": 1 - c}, device_id_type=MESH_ID)
    pl.semaphore_wait(barrier, 2 * (chips - 1) + 3 * (lines - 1) + 1)

    def beside(s):
        return s + 1 - 2 * (s % 2)

    def above(s):
        return (s + 2) % 4

    def store(p):
        return (r.wq, r.wo, r.wf, r.wp)[p]

    def source(p):
        return (r.wq_in, r.wo_in, r.wf_in, r.wp_in)[p]

    def height(p):
        return source(p).shape[0]

    def core_half(p, s, core):
        return store(p).at[s, row_block(core, height(p) // 2)]

    def first_hop(p, s, neighbour, which):
        return remote(
            source(p).at[row_block(c, height(p) // 2)],
            core_half(p, s, c),
            r.w_first_s.at[p, which],
            r.w_first_r.at[s, p],
            section=neighbour,
        )

    def second_hop(p, s, which):
        view = store(p).at[s, row_block(2 * c + which, height(p) // 4)]
        return remote(
            view, view, r.w_second_s.at[s, p], r.w_second_r.at[s, p, which], section=3 - s
        )

    def core_hop(p, s, core):
        view = core_half(p, s, core)
        return remote(view, view, r.w_core_s.at[s, p], r.w_core_r.at[s, p], seq=1 - c)

    def own_copy(p):
        return pltpu.make_async_copy(source(p), store(p).at[a], r.w_own.at[p])

    def pass_on(s, p, which):
        line = (beside(s), above(s))[which]

        @pl.when(a == line)
        def _():
            first_hop(p, s, line, which).wait_recv()
            second_hop(p, s, which).start()
            core_hop(p, s, c).start()

    def pass_all(s, pieces):
        for p in pieces:
            for which in range(2):
                pass_on(s, p, which)

    def pass_far(s, p):
        @pl.when(a == 3 - s)
        def _():
            second_hop(p, s, 0).wait_recv()
            second_hop(p, s, 1).wait_recv()
            core_hop(p, s, c).start()

    def need(s, p):
        @pl.when(s == 0)
        def _():
            if p < 2:
                pass_all(0, (p,))
            pass_far(0, p)

        @pl.when(a == s)
        def _():
            own_copy(p).wait()

        @pl.when(a != s)
        def _():
            core_hop(p, s, 1 - c).wait_recv()

    def small_copy(step, line, slot):
        return remote(
            r.small_own, r.small.at[slot], r.small_s.at[step], r.small_r.at[slot], section=line
        )

    def count_copy(step, line, slot):
        return remote(
            r.count_own.at[line],
            r.count.at[slot],
            r.count_s.at[step],
            r.count_r.at[slot],
            section=line,
        )

    singles = (r.ln1_gain, r.ln1_shift, r.ln2_gain, r.ln2_shift, r.b_out, r.b_proj)
    for place, single in enumerate(singles):
        r.small_own[place : place + 1] = single[...]
    r.small_own[6:7, :units] = r.b_fc[...]
    r.small_own[7:8, :head_width] = r.b_qv[0:1]
    r.small_own[7:8, half_width : half_width + head_width] = r.b_qv[1:2]
    for step in range(1, lines):
        small_copy(step - 1, (a + step) % lines, a).start()

    def send_pieces(pieces):
        for p in pieces:
            for which, line in enumerate((beside(a), above(a))):
                first_hop(p, a, line, which).start()

    r.small[a] = r.small_own[...]

    def place_of(index):
        inside = index % local
        stream, left = inside // stream_rows, inside % stream_rows
        first = (index // local) * local + (left // owned) * (local // 2)
        return first + stream * owned + left % owned

    def iota(shape, dimension):
        return lax.broadcasted_iota(jnp.int32, shape, dimension)

    square = jnp.where(iota((KSEL, KSEL), 0) == iota((KSEL, KSEL), 1), 1.0, 0.0).astype(LOW)
    position = place_of(iota((KSEL, total), 1)).astype(F32)
    for pair in range(lines * heads):
        line, head = pair // heads, pair % heads
        columns = dot_nt(square, r.chosen[pair].astype(F32).astype(LOW))
        for block in range(blocks):
            pick = head * blocks + block
            r.count_own[line, pick : pick + 1, :] = jnp.sum(
                jnp.where(columns[:, block : block + 1] == position, 1.0, 0.0),
                axis=0,
                keepdims=True,
            )
    for step in range(1, lines):
        count_copy(step - 1, (a + step) % lines, a).start()
    r.count[a] = r.count_own[a]

    NEAR, OVER, ACROSS = range(3)

    def gather(buffer, s, kind, j, owner, target, slot):
        view = buffer.at[s, j, row_block(owner - 1, owned)]
        return remote(
            view, view, r.ag_s.at[kind, j, slot], r.ag_r.at[kind, j, slot], tensor=target
        )

    def gather_start(buffer, s, kind, j):
        gather(buffer, s, kind, j, t, over_chip, OVER).start()
        gather(buffer, s, kind, j, t, across_chip, ACROSS).start()
        gather(buffer, s, kind, j, t, near_chip, NEAR).start()

    def gather_wait(buffer, s, kind, j):
        @pl.when(middle_chip)
        def _():
            gather(buffer, s, kind, j, across_chip, across_chip, ACROSS).wait_recv()

        @pl.when(end_chip)
        def _():
            gather(buffer, s, kind, j, near_chip, near_chip, NEAR).wait_recv()
            gather(buffer, s, kind, j, over_chip, over_chip, OVER).wait_recv()

    def gather_sent(buffer, s, kind, j):
        @pl.when(middle_chip)
        def _():
            gather(buffer, s, kind, j, t, over_chip, OVER).wait_send()
            gather(buffer, s, kind, j, t, across_chip, ACROSS).wait_send()
            gather(buffer, s, kind, j, t, near_chip, NEAR).wait_send()

    def scatter(s, kind, j, owner, slot):
        return remote(
            r.part.at[kind, j, row_block(owner - 1, owned)],
            r.arrived.at[s, kind, j, slot],
            r.rs_s.at[kind, j, slot],
            r.rs_r.at[kind, j, slot],
            tensor=owner,
        )

    def scatter_start(s, kind, j, product):
        r.part[kind, j] = product.astype(LOW)

        @pl.when(end_chip)
        def _():
            scatter(s, kind, j, over_chip, OVER).start()
            scatter(s, kind, j, near_chip, NEAR).start()

        @pl.when(middle_chip)
        def _():
            scatter(s, kind, j, across_chip, ACROSS).start()

    def scatter_sum(s, kind, j):
        result = r.part[kind, j, mine].astype(F32)
        for slot in (NEAR, ACROSS, OVER):
            scatter(s, kind, j, t, slot).wait_recv()
            result = result + r.arrived[s, kind, j, slot].astype(F32)
        return result

    def scatter_sent(s, kind, j):
        @pl.when(end_chip)
        def _():
            scatter(s, kind, j, over_chip, OVER).wait_send()
            scatter(s, kind, j, near_chip, NEAR).wait_send()

        @pl.when(middle_chip)
        def _():
            scatter(s, kind, j, across_chip, ACROSS).wait_send()

    own_rows = (r.nrm, r.nmlp, r.ups, r.brn, r.act, r.gpre, r.mix, r.dqkv)
    all_rows = (
        r.all_nrm,
        r.all_nmlp,
        r.all_ups,
        r.all_brn,
        r.all_act,
        r.all_gpre,
        r.all_mix,
        r.all_dqkv,
    )

    def rows_copy(index, s, same, stays=False):
        core = c if same else 1 - c
        src = own_rows[index].at[s]
        dst = all_rows[index].at[a, c]
        if index <= BRN:
            src = src.at[:, :, row_block(core, half_width)]
        recv = r.rows_r.at[index]
        if stays:
            return pltpu.make_async_copy(src, dst, recv)
        if same:
            return remote(src, dst, r.rows_s.at[index, s, 0], recv, section=s)
        return remote(src, dst, r.rows_s.at[index, s, 1], recv, section=s, seq=1 - c)

    def rows_start(index, s):
        @pl.when(a == s)
        def _():
            rows_copy(index, s, True, True).start()

        @pl.when(a != s)
        def _():
            rows_copy(index, s, True).start()

        if index <= BRN:
            rows_copy(index, s, False).start()

    def forward_rows(s):
        for index in (NRM, MIX, NMLP, ACT):
            rows_start(index, s)

    def rows_sent(index, s):
        @pl.when(a != s)
        def _():
            rows_copy(index, s, True).wait_send()

        if index <= BRN:
            rows_copy(index, s, False).wait_send()

    def share_copy(index, core):
        view = all_rows[index].at[:, core]
        return remote(view, view, r.share_s.at[index - ACT], r.share_r.at[index - ACT], seq=1 - c)

    def share(index):
        drain(all_rows[index].at[:, c], r.rows_r.at[index])
        share_copy(index, c).start()

    def norm_copy(s):
        return remote(
            r.norm_part.at[s], r.norm_all.at[a], r.norm_s.at[s], r.norm_r, section=s
        )

    def norm_start(s):
        @pl.when(a == s)
        def _():
            pltpu.make_async_copy(r.norm_part.at[s], r.norm_all.at[a], r.norm_r).start()

        @pl.when(a != s)
        def _():
            norm_copy(s).start()

    def home_copy(what, s, chip):
        src, dst, send, recv = what
        return remote(
            src.at[s, chip % 2],
            dst.at[a],
            send.at[s, chip % 2],
            recv,
            section=s,
            tensor=chip,
        )

    def home_start(what, s):
        src, dst, send, recv = what

        @pl.when(middle_chip & (a == s))
        def _():
            pltpu.make_async_copy(src.at[s, t % 2], dst.at[a], recv).start()

        @pl.when(middle_chip & (a != s))
        def _():
            home_copy(what, s, t).start()

        @pl.when(middle_chip)
        def _():
            home_copy(what, s, near_chip).start()

    def home_sent(what, s):
        @pl.when(middle_chip & (a != s))
        def _():
            home_copy(what, s, t).wait_send()

        @pl.when(middle_chip)
        def _():
            home_copy(what, s, near_chip).wait_send()

    out_home = (r.out_low, r.acts, r.out_s, r.out_r)
    grad_home = (r.grad_low, r.grads, r.grad_s, r.grad_r)

    length = r.lengths[a // buckets, a % buckets]
    key = place_of(iota((stream_rows, total), 1))
    for j in streams:
        query = place_of(c * local + j * stream_rows + iota((stream_rows, total), 0))
        r.near[j] = jnp.where((query >= key) & (query - key < WIN), 1.0, 0.0)
    key_row = place_of(iota((1, total), 1))

    def row_mask(place):
        return jnp.where(place < length, 1.0, 0.0)

    def multiplicity(s, j, head):
        far = []
        for block in range(blocks):
            pick = head * blocks + block
            limit = (c * blocks + block) * QB - WIN
            counted = jnp.where(key_row <= limit, r.count[s, pick : pick + 1, :], 0.0)
            far.append(jnp.broadcast_to(counted, (stream_rows // blocks, total)))
        return r.near[j] + jnp.concatenate(far, axis=0)

    def head_cols(head):
        return slice(head * HDIM, (head + 1) * HDIM)

    def kv_copy(s):
        view = r.kv.at[s, :, 0:local]
        return remote(view, view, r.kv_s.at[s], r.kv_r.at[s], seq=1 - c)

    def dkv_copy(s):
        return remote(r.dkv_out.at[s], r.dkv_in.at[s], r.dkv_s.at[s], r.dkv_r.at[s], seq=1 - c)

    def own_sequence(ref):
        both = ref[a // buckets].astype(F32)
        picked = both[:, 0, :]
        for bucket in range(1, buckets):
            picked = jnp.where(a % buckets == bucket, both[:, bucket, :], picked)
        return picked

    def own_part(j):
        chip, first = (j * owned) // rows, (j * owned) % rows
        return chip, slice(first, first + owned)

    def first_copy():
        return remote(r.first_out, r.first_in, r.first_s, r.first_r, tensor=near_chip)

    own_place = c * local + t * rows + iota((rows, 1), 0)
    r.first_out[0] = own_sequence(r.inputs).astype(LOW)
    r.first_out[1] = (own_sequence(r.cotangent) * row_mask(own_place)).astype(LOW)
    r.norm_part[...] = jnp.zeros_like(r.norm_part)

    @pl.when(c == 0)
    def _():
        r.kv[:, :, local:total] = jnp.zeros((lines, 2, local, head_width), LOW)


    @pl.when(end_chip)
    def _():
        first_copy().start()

    @pl.when(middle_chip)
    def _():
        first_copy().wait_recv()
        for which in range(2):
            here, beside_it = r.first_out[which].astype(F32), r.first_in[which].astype(F32)
            lower = jnp.where(t % 2 == 0, here, beside_it)
            upper = jnp.where(t % 2 == 0, beside_it, here)
            for j in streams:
                chip, part = own_part(j)
                own_block = (lower, upper)[chip][part]
                if which == 0:
                    r.hidden[j] = own_block
                else:
                    r.upstream[j] = own_block.astype(LOW)

    def on_owner(stage):
        def run(s, j):
            @pl.when(middle_chip)
            def _():
                stage(s, j)

        return run

    def keep_rows(target, s, j, result):
        chip, part = own_part(j)
        target[s, chip, part] = result

    @on_owner
    def enter(s, j):
        xhat, inverse = standard(r.hidden[j])
        r.xhat1[s, j] = xhat
        r.inv1[s, j] = jnp.broadcast_to(inverse, (owned, 128))
        r.nrm[s, j, mine] = (xhat * r.small[s, 0:1] + r.small[s, 1:2]).astype(LOW)
        gather_start(r.nrm, s, 0, j)

    def project(s, j):
        gather_wait(r.nrm, s, 0, j)
        normed = r.nrm[s, j]
        place = row_block(c * STREAMS + j, stream_rows)
        bias_v = r.small[s, 7:8, half_width : half_width + head_width]
        key_rows = dot_nt(normed, r.wq[s, head_width : 2 * head_width])
        value_rows = dot_nt(normed, r.wq[s, 2 * head_width : 3 * head_width]) + bias_v
        r.kv[s, 0, place] = key_rows.astype(LOW)
        r.kv[s, 1, place] = value_rows.astype(LOW)
        gather_sent(r.nrm, s, 0, j)

    def ask(s, j):
        queries = dot_nt(r.nrm[s, j], r.wq[s, 0:head_width]) + r.small[s, 7:8, :head_width]
        r.qry[s, j] = queries.astype(LOW)

    def attend_line(s, j):
        mixed = []
        for head in range(heads):
            cols = head_cols(head)
            times = multiplicity(s, j, head)
            scores = scale * dot_nt(r.qry[s, j, :, cols], r.kv[s, 0, :, cols])
            scores = jnp.where(times > 0.0, scores, MASKED)
            top = jnp.max(scores, axis=-1, keepdims=True)
            terms = times * jnp.exp(scores - top)
            weights = terms / jnp.sum(terms, axis=-1, keepdims=True)
            r.soft[s, j, head] = weights
            mixed.append(dot_nn(weights.astype(LOW), r.kv[s, 1, :, cols]))
        mask = row_mask(place_of(c * local + j * stream_rows + iota((stream_rows, 1), 0)))
        r.mix[s, j] = (jnp.concatenate(mixed, axis=-1) * mask).astype(LOW)

    def leave_attention(s, j):
        scatter_start(s, 0, j, dot_nn(r.mix[s, j], r.wo[s]))

    @on_owner
    def between(s, j):
        middle = r.hidden[j] + scatter_sum(s, 0, j) + r.small[s, 4:5]
        r.middle[j] = middle
        xhat, inverse = standard(middle)
        r.xhat2[s, j] = xhat
        r.inv2[s, j] = jnp.broadcast_to(inverse, (owned, 128))
        r.nmlp[s, j, mine] = (xhat * r.small[s, 2:3] + r.small[s, 3:4]).astype(LOW)
        gather_start(r.nmlp, s, 1, j)

    def feed(s, j):
        gather_wait(r.nmlp, s, 1, j)
        before = dot_nn(r.nmlp[s, j], r.wf[s]) + r.small[s, 6:7, :units]
        bend = jnp.tanh(0.7978845608028654 * (before + 0.044715 * before * before * before))
        r.act[s, j] = (0.5 * before * (1.0 + bend)).astype(LOW)
        r.slope[s, j] = 0.5 * (1.0 + bend) + 0.5 * before * (1.0 - bend * bend) * (
            0.7978845608028654 * (1.0 + 3 * 0.044715 * before * before)
        )

        gather_sent(r.nmlp, s, 1, j)

    def leave_feed(s, j):
        scatter_start(s, 1, j, dot_nn(r.act[s, j], r.wp[s]))

    @on_owner
    def finish(s, j):
        result = r.middle[j] + scatter_sum(s, 1, j) + r.small[s, 5:6]
        keep_rows(r.out_low, s, j, result.astype(LOW))
        r.hidden[j] = result.astype(LOW).astype(F32)

    def small_ready(s):
        @pl.when(a != s)
        def _():
            small_copy(0, a, s).wait_recv()

    small_ready(0)
    for j in streams:
        enter(0, j)

    @pl.when(a == 0)
    def _():
        send_pieces(range(4))

    @pl.when(a != 0)
    def _():
        send_pieces((0, 1))

    for p in range(4):
        own_copy(p).start()

    def forward(s, _):
        need(s, 0)
        for j in streams:
            project(s, j)

        @pl.when(c == 0)
        def _():
            kv_copy(s).start()

        for j in streams:
            ask(s, j)

        @pl.when(a != s)
        def _():
            count_copy(0, a, s).wait_recv()

        @pl.when(c == 1)
        def _():
            kv_copy(s).wait_recv()

        for j in streams:
            attend_line(s, j)
            if j == 0:
                need(s, 1)
            leave_attention(s, j)

        @pl.when(s == 0)
        def _():
            for later in range(1, lines):
                pass_all(later, (0, 1))

        @pl.when(s == 1)
        def _():
            pass_all(1, (3,))
            pass_far(1, 2)
            for later in range(2, lines):
                pass_far(later, 0)
                pass_far(later, 1)

        @pl.when(s == 2)
        def _():
            pass_far(2, 3)
            pass_far(3, 3)

        for j in streams:
            between(s, j)
            scatter_sent(s, 0, j)
        @pl.when(s == 0)
        def _():
            pass_all(0, (2,))

        @pl.when((s == 0) & (a != 0))
        def _():
            send_pieces((2,))

        @pl.when((s == 1) & (a >= 2))
        def _():
            send_pieces((3,))

        need(s, 2)
        for j in streams:
            feed(s, j)
            if j == 0:

                @pl.when(s == 0)
                def _():
                    pass_all(0, (3,))

                @pl.when(s == 1)
                def _():
                    pass_far(1, 3)

                need(s, 3)
            leave_feed(s, j)


        @pl.when((s == 0) & (a == 1))
        def _():
            send_pieces((3,))

        @pl.when(s >= 2)
        def _():
            forward_rows(s - 2)


        @pl.when(s + 1 < lines)
        def _():
            small_ready(s + 1)

        for j in streams:
            finish(s, j)
            scatter_sent(s, 1, j)

            @pl.when(s + 1 < lines)
            def _():
                enter(s + 1, j)

        home_start(out_home, s)

        @pl.when(s == 0)
        def _():
            for later in range(1, lines):
                pass_all(later, (2,))
            pass_far(1, 0)
            pass_far(1, 1)

        @pl.when(s == 1)
        def _():
            for later in range(2, lines):
                pass_all(later, (3,))
                pass_far(later, 2)

        return 0

    lax.fori_loop(0, lines, forward, 0)

    @on_owner
    def turn(s, j):
        upstream = r.upstream[j]
        r.ups[s, j, mine] = upstream
        gather_start(r.ups, s, 2, j)
        r.norm_part[s, 5:6] += column_sum(upstream)

    def feed_back(s, j):
        gather_wait(r.ups, s, 2, j)
        grad_pre = (dot_nt(r.ups[s, j], r.wp[s]) * r.slope[s, j]).astype(LOW)
        r.gpre[s, j] = grad_pre
        scatter_start(s, 2, j, dot_nt(grad_pre, r.wf[s]))
        r.norm_part[s, 6:7, :units] += column_sum(grad_pre)
        gather_sent(r.ups, s, 2, j)

    @on_owner
    def between_back(s, j):
        grad = scatter_sum(s, 2, j)
        xhat = r.xhat2[s, j]
        upstream = r.upstream[j].astype(F32)
        grad_middle = upstream + standard_back(
            grad * r.small[s, 2:3], xhat, r.inv2[s, j, :, 0:1]
        )
        r.middle[j] = grad_middle
        branch = grad_middle.astype(LOW)
        r.brn[s, j, mine] = branch
        gather_start(r.brn, s, 3, j)
        r.norm_part[s, 2:3] += column_sum(grad * xhat)
        r.norm_part[s, 3:4] += column_sum(grad)
        r.norm_part[s, 4:5] += column_sum(branch)

    def mixed_back(s, j):
        gather_wait(r.brn, s, 3, j)
        place = place_of(c * local + j * stream_rows + iota((stream_rows, 1), 0))
        r.gmix[j] = (dot_nt(r.brn[s, j], r.wo[s]) * row_mask(place)).astype(LOW)
        gather_sent(r.brn, s, 3, j)

    def attend_line_back(s, j):
        grad_q, grad_k, grad_v = [], [], []
        for head in range(heads):
            cols = head_cols(head)
            weights = r.soft[s, j, head]
            grad_head = r.gmix[j, :, cols]
            grad_weights = dot_nt(grad_head, r.kv[s, 1, :, cols])
            inner = jnp.sum(weights * grad_weights, axis=-1, keepdims=True)
            grad_scores = (weights * (grad_weights - inner)).astype(LOW)
            grad_k.append(scale * dot_tn(grad_scores, r.qry[s, j, :, cols]))
            grad_v.append(dot_tn(weights.astype(LOW), grad_head))
            grad_q.append(scale * dot_nn(grad_scores, r.kv[s, 0, :, cols]))
        for which, grad in enumerate((grad_k, grad_v)):
            grad = jnp.concatenate(grad, axis=-1)
            r.dkv_all[which] = grad if j == 0 else r.dkv_all[which] + grad
        grad_q = jnp.concatenate(grad_q, axis=-1).astype(LOW)
        r.dqkv[s, 0, j] = grad_q
        r.norm_part[s, 7:8, :head_width] += column_sum(grad_q)

    def join_keys(s):
        @pl.when(c == 1)
        def _():
            r.dkv_out[s] = r.dkv_all[:, 0:local].astype(LOW)
            dkv_copy(s).start()

        @pl.when(c == 0)
        def _():
            dkv_copy(s).wait_recv()
            r.dkv_all[:, 0:local] += r.dkv_in[s].astype(F32)

        for which in range(2):
            joined = r.dkv_all[which, my_half].astype(LOW)
            r.dqkv[s, 1 + which] = joined.reshape(r.dqkv.shape[2:])
            if which == 1:
                r.norm_part[s, 7:8, half_width : half_width + head_width] = column_sum(joined)

    def leave_back(s, j):
        product = dot_nn(r.dqkv[s, 0, j], r.wq[s, 0:head_width])
        for which in range(1, 3):
            weight = r.wq[s, which * head_width : (which + 1) * head_width]
            product = product + dot_nn(r.dqkv[s, which, j], weight)
        scatter_start(s, 3, j, product)

    @on_owner
    def finish_back(s, j):
        grad = scatter_sum(s, 3, j)
        xhat = r.xhat1[s, j]
        result = r.middle[j] + standard_back(
            grad * r.small[s, 0:1], xhat, r.inv1[s, j, :, 0:1]
        )
        r.upstream[j] = result.astype(LOW)
        keep_rows(r.grad_low, s, j, result.astype(LOW))
        r.norm_part[s, 0:1] += column_sum(grad * xhat)
        r.norm_part[s, 1:2] += column_sum(grad)

    for j in streams:
        turn(lines - 1, j)

    def backward(index, _):
        s = lines - 1 - index
        for j in streams:
            feed_back(s, j)
        rows_start(UPS, s)
        rows_start(GPRE, s)

        @pl.when(index < 2)
        def _():
            forward_rows(lines - 2 + index)

        @pl.when(index == lines - 1)
        def _():
            share(ACT)
            share(MIX)

        for j in streams:
            between_back(s, j)
            scatter_sent(s, 2, j)
        for j in streams:
            mixed_back(s, j)
            attend_line_back(s, j)
        join_keys(s)
        rows_start(BRN, s)
        for j in streams:
            leave_back(s, j)
        rows_start(DQKV, s)
        for j in streams:
            finish_back(s, j)
            scatter_sent(s, 3, j)

            @pl.when(s > 0)
            def _():
                turn(s - 1, j)

        norm_start(s)
        home_start(grad_home, s)
        return 0

    lax.fori_loop(0, lines, backward, 0)

    share(GPRE)
    share(DQKV)

    drain(r.norm_all, r.norm_r)
    slot = c * chips + t
    norm_sum = r.norm_all[0]
    for line in range(1, lines):
        norm_sum = norm_sum + r.norm_all[line]
    r.ends[slot] = norm_sum

    def ends_copy(step):
        core, chip = step // chips, step % chips
        view = r.ends.at[slot]
        return remote(
            view,
            view,
            r.ends_s.at[step - 1],
            r.ends_r,
            seq=(c + core) % 2,
            tensor=(t + chip) % chips,
        )

    for step in range(1, 2 * chips):
        ends_copy(step).start()

    for index in range(ACT):
        drain(all_rows[index], r.rows_r.at[index])
    for index in range(ACT, 8):
        share_copy(index, 1 - c).wait_recv()
        share_copy(index, c).wait_send()
    drain(r.acts, r.out_r)
    drain(r.grads, r.grad_r)
    drain(r.ends.at[0 : 2 * chips - 1], r.ends_r)
    for step in range(1, 2 * chips):
        ends_copy(step).wait_send()
    for step in range(1, lines):
        small_copy(step - 1, (a + step) % lines, a).wait_send()
        count_copy(step - 1, (a + step) % lines, a).wait_send()
    for p in range(4):
        for which, line in enumerate((beside(a), above(a))):
            first_hop(p, a, line, which).wait_send()

    @pl.when(end_chip)
    def _():
        first_copy().wait_send()

    def sent(s, _):
        home_sent(out_home, s)
        home_sent(grad_home, s)

        @pl.when(a != s)
        def _():
            norm_copy(s).wait_send()

        @pl.when(c == 0)
        def _():
            kv_copy(s).wait_send()

        @pl.when(c == 1)
        def _():
            dkv_copy(s).wait_send()

        for index in range(8):
            rows_sent(index, s)
        for p in range(4):

            @pl.when((a == beside(s)) | (a == above(s)))
            def _():
                second_hop(p, s, 0).wait_send()

            @pl.when(a != s)
            def _():
                core_hop(p, s, c).wait_send()

        return 0

    lax.fori_loop(0, lines, sent, 0)


def relay_call(inputs, cotangent, lengths, chosen, singles, weights):
    lines = lax.axis_size("section")
    chips = lax.axis_size("tensor")
    rows, buckets, width = inputs.shape[1:]
    local, total, half = rows * chips, 2 * rows * chips, width // 2
    head_width, units = weights["wo_in"].shape[0], weights["wp_in"].shape[0]
    heads = head_width // HDIM
    stream = local // STREAMS
    peers, owned = chips - 1, stream // 2
    vmem, dma = pltpu.VMEM, pltpu.SemaphoreType.DMA
    operands = dict(
        inputs=inputs,
        cotangent=cotangent,
        lengths=lengths,
        chosen=chosen,
        **singles,
        **weights,
    )

    def space(name):
        if name in weights:
            return pl.ANY
        return pltpu.SMEM if operands[name] is lengths else pltpu.VMEM

    sums = dict(
        acts=((lines, rows, width), LOW),
        grads=((lines, rows, width), LOW),
        ends=((2 * chips, 8, width), F32),
    )
    gathered = dict(
        all_nrm=((lines, 2, STREAMS, stream, half), LOW),
        all_nmlp=((lines, 2, STREAMS, stream, half), LOW),
        all_ups=((lines, 2, STREAMS, stream, half), LOW),
        all_brn=((lines, 2, STREAMS, stream, half), LOW),
        all_act=((lines, 2, STREAMS, stream, units), LOW),
        all_gpre=((lines, 2, STREAMS, stream, units), LOW),
        all_mix=((lines, 2, STREAMS, stream, head_width), LOW),
        all_dqkv=((lines, 2, 3, STREAMS, stream, head_width), LOW),
    )
    outputs = dict(**sums, **gathered)
    scratch = dict(
        wq=vmem((lines,) + weights["wq_in"].shape, LOW),
        wo=vmem((lines,) + weights["wo_in"].shape, LOW),
        wf=vmem((lines,) + weights["wf_in"].shape, LOW),
        wp=vmem((lines,) + weights["wp_in"].shape, LOW),
        small_own=vmem((8, width), F32),
        small=vmem((lines, 8, width), F32),
        count_own=vmem((lines, 8, total), F32),
        count=vmem((lines, 8, total), F32),
        hidden=vmem((STREAMS, owned, width), F32),
        middle=vmem((STREAMS, owned, width), F32),
        upstream=vmem((STREAMS, owned, width), LOW),
        first_out=vmem((2, rows, width), LOW),
        first_in=vmem((2, rows, width), LOW),
        xhat1=vmem((lines, STREAMS, owned, width), F32),
        inv1=vmem((lines, STREAMS, owned, 128), F32),
        xhat2=vmem((lines, STREAMS, owned, width), F32),
        inv2=vmem((lines, STREAMS, owned, 128), F32),
        nrm=vmem((lines, STREAMS, stream, width), LOW),
        nmlp=vmem((lines, STREAMS, stream, width), LOW),
        ups=vmem((lines, STREAMS, stream, width), LOW),
        brn=vmem((lines, STREAMS, stream, width), LOW),
        act=vmem((lines, STREAMS, stream, units), LOW),
        gpre=vmem((lines, STREAMS, stream, units), LOW),
        slope=vmem((lines, STREAMS, stream, units), F32),
        mix=vmem((lines, STREAMS, stream, head_width), LOW),
        qry=vmem((lines, STREAMS, stream, head_width), LOW),
        gmix=vmem((STREAMS, stream, head_width), LOW),
        dqkv=vmem((lines, 3, STREAMS, stream, head_width), LOW),
        kv=vmem((lines, 2, total, head_width), LOW),
        soft=vmem((lines, STREAMS, heads, stream, total), F32),
        near=vmem((STREAMS, stream, total), F32),
        dkv_all=vmem((2, total, head_width), F32),
        dkv_out=vmem((lines, 2, local, head_width), LOW),
        dkv_in=vmem((lines, 2, local, head_width), LOW),
        part=vmem((4, STREAMS, stream, width), LOW),
        arrived=vmem((lines, 4, STREAMS, peers, owned, width), LOW),
        out_low=vmem((lines, 2, rows, width), LOW),
        grad_low=vmem((lines, 2, rows, width), LOW),
        norm_part=vmem((lines, 8, width), F32),
        norm_all=vmem((lines, 8, width), F32),
        w_first_s=dma((4, 2)),
        w_first_r=dma((lines, 4)),
        w_second_s=dma((lines, 4)),
        w_second_r=dma((lines, 4, 2)),
        w_core_s=dma((lines, 4)),
        w_core_r=dma((lines, 4)),
        w_own=dma((4,)),
        small_s=dma((lines - 1,)),
        small_r=dma((lines,)),
        count_s=dma((lines - 1,)),
        count_r=dma((lines,)),
        ag_s=dma((4, STREAMS, peers)),
        ag_r=dma((4, STREAMS, peers)),
        rs_s=dma((4, STREAMS, peers)),
        rs_r=dma((4, STREAMS, peers)),
        kv_s=dma((lines,)),
        kv_r=dma((lines,)),
        dkv_s=dma((lines,)),
        dkv_r=dma((lines,)),
        rows_s=dma((8, lines, 2)),
        rows_r=dma((8,)),
        share_s=dma((4,)),
        share_r=dma((4,)),
        first_s=dma,
        first_r=dma,
        out_s=dma((lines, 2)),
        out_r=dma,
        grad_s=dma((lines, 2)),
        grad_r=dma,
        norm_s=dma((lines,)),
        norm_r=dma,
        ends_s=dma((2 * chips - 1,)),
        ends_r=dma,
    )
    names = tuple(operands) + tuple(outputs) + tuple(scratch)
    results = pl.pallas_call(
        functools.partial(relay_kernel, names),
        out_shape=[jax.ShapeDtypeStruct(shape, kind) for shape, kind in outputs.values()],
        in_specs=[pl.BlockSpec(memory_space=space(name)) for name in operands],
        out_specs=[
            pl.BlockSpec(memory_space=pl.ANY if name in gathered else pltpu.VMEM)
            for name in outputs
        ],
        scratch_shapes=list(scratch.values()),
        compiler_params=pltpu.CompilerParams(
            collective_id=0, has_side_effects=True, vmem_limit_bytes=60 * 2**20
        ),
        name="relay",
    )(*operands.values())
    return dict(zip(outputs, results))


def weights_kernel(names, *refs):
    r = types.SimpleNamespace(**dict(zip(names, refs)))
    step = pl.program_id(0)
    micro_count, rows, buckets, width = r.activations.shape
    chips, units, head_width = r.ends.shape[0] // 2, r.all_act.shape[-1], r.all_mix.shape[-1]

    @pl.when(step == 0)
    def _():
        sums = r.ends[0]
        for other in range(1, 2 * chips):
            sums = sums + r.ends[other]
        singles = (r.ln1_gain, r.ln1_shift, r.ln2_gain, r.ln2_shift, r.b_out, r.b_proj)
        for place, single in enumerate(singles):
            single[...] = sums[place : place + 1]
        for chip in range(chips):
            both = r.ends[chip] + r.ends[chips + chip]
            r.b_fc[:, chip * units : (chip + 1) * units] = both[6:7, :units]
            here = slice(chip * head_width, (chip + 1) * head_width)
            r.b_qv[0:1, here] = both[7:8, :head_width]
            r.b_qv[1:2, here] = both[7:8, width // 2 : width // 2 + head_width]
        for target, source in ((r.activations, r.acts), (r.in_grads, r.grads)):
            for micro in range(micro_count):
                rows_of = [
                    source[micro * buckets + bucket].astype(F32)[:, None, :]
                    for bucket in range(buckets)
                ]
                target[micro] = jnp.concatenate(rows_of, axis=1).astype(LOW)
        for target in (r.w_qkv, r.w_out, r.w_fc, r.w_proj):
            target[...] = jnp.zeros_like(target)

    def rows_of_sequence(ref):
        return ref[0].reshape(2 * chips * rows, ref.shape[-1])

    nrm, nmlp, ups, brn, act, gpre, mix = (
        rows_of_sequence(ref)
        for ref in (r.all_nrm, r.all_nmlp, r.all_ups, r.all_brn, r.all_act, r.all_gpre, r.all_mix)
    )
    r.w_proj[...] += dot_tn(act, ups)
    r.w_fc[...] += dot_tn(nmlp, gpre)
    r.w_out[...] += dot_tn(mix, brn)
    for which in range(3):
        grad = r.all_dqkv[0, :, which].reshape(2 * chips * rows, head_width)
        r.w_qkv[which] += dot_tn(grad, nrm)


def weights_call(relayed, inputs_shape, head_width, units):
    lines = lax.axis_size("section")
    chips = lax.axis_size("tensor")
    width = inputs_shape[-1]
    half = width // 2
    outputs = dict(
        activations=(inputs_shape, LOW),
        in_grads=(inputs_shape, LOW),
        ln1_gain=((1, width), F32),
        ln1_shift=((1, width), F32),
        w_qkv=((3, head_width, half), F32),
        b_qv=((2, width), F32),
        w_out=((head_width, half), F32),
        b_out=((1, width), F32),
        ln2_gain=((1, width), F32),
        ln2_shift=((1, width), F32),
        w_fc=((half, units), F32),
        b_fc=((1, chips * units), F32),
        w_proj=((units, half), F32),
        b_proj=((1, width), F32),
    )

    def spec(array):
        if len(array.shape) < 5:
            return pl.BlockSpec(array.shape, lambda step: (0,) * len(array.shape))
        return pl.BlockSpec(
            (1,) + array.shape[1:], lambda step: (step,) + (0,) * (len(array.shape) - 1)
        )

    def whole(shape):
        return pl.BlockSpec(shape, lambda step: (0,) * len(shape))

    return pl.pallas_call(
        functools.partial(weights_kernel, tuple(relayed) + tuple(outputs)),
        out_shape=[jax.ShapeDtypeStruct(shape, kind) for shape, kind in outputs.values()],
        grid=(lines,),
        in_specs=[spec(array) for array in relayed.values()],
        out_specs=[whole(shape) for shape, _ in outputs.values()],
        compiler_params=pltpu.CompilerParams(vmem_limit_bytes=60 * 2**20),
        name="weight_gradients",
    )(*relayed.values())


def on_line(
    inputs,
    cotangent,
    lengths,
    chosen,
    ln1_gain,
    ln1_shift,
    w_qkv,
    b_qv,
    w_out,
    b_out,
    ln2_gain,
    ln2_shift,
    w_fc,
    b_fc,
    w_proj,
    b_proj,
):
    head_width, units = w_out.shape[1], w_fc.shape[2]
    singles = dict(
        ln1_gain=ln1_gain,
        ln1_shift=ln1_shift,
        ln2_gain=ln2_gain,
        ln2_shift=ln2_shift,
        b_out=b_out,
        b_proj=b_proj,
        b_fc=b_fc,
        b_qv=b_qv[0],
    )
    weights = dict(
        wq_in=jnp.swapaxes(w_qkv[0], 1, 2).reshape(-1, inputs.shape[-1]),
        wo_in=w_out[0],
        wf_in=w_fc[0],
        wp_in=w_proj[0],
    )
    picks = chosen.reshape((-1,) + chosen.shape[-2:])
    relayed = relay_call(inputs, cotangent, lengths, picks, singles, weights)
    results = list(weights_call(relayed, inputs.shape, head_width, units))
    results[4] = jnp.swapaxes(results[4], 1, 2)
    vectors = (2, 3, 7, 8, 9, 11, 13)
    return tuple(
        result if place in vectors else result[None] for place, result in enumerate(results)
    )


def fits_lines(mesh):
    return mesh.shape["section"] == 4 and mesh.shape["seq"] == 2 and mesh.shape["tensor"] == 4


def solution(mesh):
    placed = (
        P(None, ("seq", "tensor"), None, None),
        P(None, ("seq", "tensor"), None, None),
        P(),
        P("section", None, None, "tensor", "seq", None),
        P("section", None),
        P("section", None),
        P("section", None, None, "tensor"),
        P("section", None, "tensor"),
        P("section", "tensor", None),
        P("section", None),
        P("section", None),
        P("section", None),
        P("section", None, "tensor"),
        P("section", "tensor"),
        P("section", "tensor", None),
        P("section", None),
    )
    return jax.shard_map(
        on_line if fits_lines(mesh) else on_device,
        mesh=mesh,
        in_specs=placed,
        out_specs=(
            P("section", None, ("seq", "tensor"), None, None),
            P("section", None, ("seq", "tensor"), None, None),
            P("section", None),
            P("section", None),
            P("section", None, "seq", "tensor"),
            P("section", None, None),
            P("section", "tensor", "seq"),
            P("section", None),
            P("section", None),
            P("section", None),
            P("section", "seq", "tensor"),
            P("section", None),
            P("section", "tensor", "seq"),
            P("section", None),
        ),
        check_vma=False,
    )
```

```python
import functools
import types

import jax
import jax.numpy as jnp
from jax import lax
from jax.experimental import pallas as pl
from jax.experimental.pallas import tpu as pltpu
from jax.sharding import PartitionSpec as P

HDIM = 64
WIN = 64
QB = 64
KSEL = 64


NORM_EPS = 1e-05
MASKED = -1000000000.0


def from_behind(value, axis, steps):
    count = lax.axis_size(axis)
    first, last = (max(0, -steps), min(count, count - steps))
    return lax.ppermute(value, axis, [(source, source + steps) for source in range(first, last)])


def layer_norm(values, gain, shift):
    average = jnp.mean(values, axis=-1, keepdims=True)
    centred = values - average
    variance = jnp.mean(centred * centred, axis=-1, keepdims=True)
    return centred * lax.rsqrt(variance + NORM_EPS) * gain + shift


def gelu_tanh(values):
    return (
        0.5
        * values
        * (1.0 + jnp.tanh(0.7978845608028654 * (values + 0.044715 * values * values * values)))
    )


def gather_rows(row_block):
    return lax.all_gather(row_block, "tensor", axis=0, tiled=True)


def scatter_product(left_rows, weight, formula):
    return lax.psum_scatter(
        jnp.einsum(formula, left_rows, weight, preferred_element_type=jnp.float32).astype(
            jnp.bfloat16
        ),
        "tensor",
        scatter_dimension=0,
        tiled=True,
    ).astype(jnp.float32)


def near_slabs(full_rows, seq_start, seq_first, length_local):
    buckets = full_rows.shape[1]
    heads_local = full_rows.shape[2] // HDIM
    blocks = length_local // QB
    earlier = lax.dynamic_slice_in_dim(full_rows, jnp.maximum(seq_start - WIN, 0), WIN, 0)
    earlier = jnp.where(seq_first, jnp.zeros_like(earlier), earlier)
    local_part = lax.dynamic_slice_in_dim(full_rows, seq_start, length_local, 0)
    segment = jnp.concatenate([earlier, local_part], 0).reshape(
        length_local + WIN, buckets, heads_local, HDIM
    )
    return jnp.concatenate(
        [
            segment[offset_index * QB : offset_index * QB + length_local].reshape(
                blocks, QB, buckets, heads_local, HDIM
            )
            for offset_index in range(WIN // QB + 1)
        ],
        1,
    )


def far_rows(full_rows, flat_index):
    total_rows, buckets, feature_width = full_rows.shape
    heads_local = feature_width // HDIM
    return jnp.take(full_rows.reshape(total_rows * buckets * heads_local, HDIM), flat_index, axis=0)


def key_geometry(chosen_now, seq_start, blocks):
    buckets, heads_local = (chosen_now.shape[0], chosen_now.shape[1])
    bucket_ids = lax.broadcasted_iota(jnp.int32, chosen_now.shape, 0)
    head_ids = lax.broadcasted_iota(jnp.int32, chosen_now.shape, 1)
    flat_index = (chosen_now * buckets + bucket_ids) * heads_local + head_ids
    block_start = seq_start + QB * lax.broadcasted_iota(jnp.int32, (blocks, 1, 1), 0)
    query_ids = lax.broadcasted_iota(jnp.int32, (1, QB, 1), 1)
    key_ids = lax.broadcasted_iota(jnp.int32, (1, 1, WIN + QB), 2)
    distance = query_ids + WIN - key_ids
    near_ok = (distance >= 0) & (distance < WIN) & (block_start + key_ids - WIN >= 0)
    far_ok = chosen_now + WIN <= block_start.reshape(1, 1, blocks, 1)
    near_mask = jnp.broadcast_to(
        near_ok[:, None, None], (blocks, buckets, heads_local, QB, WIN + QB)
    )
    far_mask = jnp.broadcast_to(
        jnp.transpose(far_ok, (2, 0, 1, 3))[:, :, :, None, :],
        (blocks, buckets, heads_local, QB, KSEL),
    )
    return (flat_index, jnp.concatenate([near_mask, far_mask], -1))


def attention_setup(queries, key_rows, value_rows, chosen_now, seq_start, seq_first):
    length_local, buckets, feature_width = queries.shape
    heads_local = feature_width // HDIM
    blocks = length_local // QB
    query_blocks = queries.reshape(blocks, QB, buckets, heads_local, HDIM)
    flat_index, key_mask = key_geometry(chosen_now, seq_start, blocks)
    near_keys = near_slabs(key_rows, seq_start, seq_first, length_local)
    near_values = near_slabs(value_rows, seq_start, seq_first, length_local)
    far_keys = far_rows(key_rows, flat_index)
    far_values = far_rows(value_rows, flat_index)
    near_scores = jnp.einsum(
        "bqnhe,btnhe->bnhqt", query_blocks, near_keys, preferred_element_type=jnp.float32
    )
    far_scores = jnp.einsum(
        "bqnhe,nhbke->bnhqk", query_blocks, far_keys, preferred_element_type=jnp.float32
    )
    scores = jnp.where(
        key_mask, HDIM ** (-0.5) * jnp.concatenate([near_scores, far_scores], -1), MASKED
    )
    return (query_blocks, near_keys, near_values, far_keys, far_values, flat_index, scores)


def attend(queries, key_rows, value_rows, chosen_now, seq_start, seq_first):
    query_blocks, near_keys, near_values, far_keys, far_values, flat_index, scores = (
        attention_setup(queries, key_rows, value_rows, chosen_now, seq_start, seq_first)
    )
    span = WIN + QB
    row_top = jnp.max(scores, -1, keepdims=True)
    exp_terms = jnp.exp(scores - row_top)
    row_total = jnp.sum(exp_terms, -1, keepdims=True)
    softmax_low = (exp_terms / row_total).astype(jnp.bfloat16)
    near_part = jnp.einsum(
        "bnhqt,btnhe->bqnhe",
        softmax_low[..., :span],
        near_values,
        preferred_element_type=jnp.float32,
    )
    far_part = jnp.einsum(
        "bnhqk,nhbke->bqnhe",
        softmax_low[..., span:],
        far_values,
        preferred_element_type=jnp.float32,
    )
    return ((near_part + far_part).reshape(queries.shape), row_top + jnp.log(row_total))


def spread_back(near_grad, far_grad, flat_index, seq_start, seq_first, total_rows):
    blocks, span, buckets, heads_local, head_size = near_grad.shape
    length_local = blocks * QB
    feature_width = heads_local * head_size
    segment = jnp.zeros((length_local + WIN, buckets, heads_local, head_size), jnp.float32)
    for offset_index in range(WIN // QB + 1):
        piece = near_grad[:, offset_index * QB : (offset_index + 1) * QB].reshape(
            length_local, buckets, heads_local, head_size
        )
        segment = segment.at[offset_index * QB : offset_index * QB + length_local].add(piece)
    full_rows = jnp.zeros((total_rows * buckets * heads_local, head_size), jnp.float32)
    full_rows = full_rows.at[flat_index.reshape(-1)].add(far_grad.reshape(-1, head_size))
    full_rows = full_rows.reshape(total_rows, buckets, feature_width)
    local_part = segment[WIN:].reshape(length_local, buckets, feature_width)
    earlier = jnp.where(seq_first, 0.0, segment[:WIN].reshape(WIN, buckets, feature_width))
    full_rows = lax.dynamic_update_slice_in_dim(
        full_rows,
        lax.dynamic_slice_in_dim(full_rows, seq_start, length_local, 0) + local_part,
        seq_start,
        0,
    )
    earlier_start = jnp.maximum(seq_start - WIN, 0)
    full_rows = lax.dynamic_update_slice_in_dim(
        full_rows,
        lax.dynamic_slice_in_dim(full_rows, earlier_start, WIN, 0) + earlier,
        earlier_start,
        0,
    )
    return full_rows


def attend_back(
    queries, key_rows, value_rows, chosen_now, seq_start, seq_first, log_total, grad_mixed
):
    query_blocks, near_keys, near_values, far_keys, far_values, flat_index, scores = (
        attention_setup(queries, key_rows, value_rows, chosen_now, seq_start, seq_first)
    )
    span = WIN + QB
    score_scale = HDIM ** (-0.5)
    grad_blocks = grad_mixed.reshape(query_blocks.shape)
    weights_full = jnp.exp(scores - log_total)
    softmax_low = weights_full.astype(jnp.bfloat16)
    grad_near_weights = jnp.einsum(
        "bqnhe,btnhe->bnhqt", grad_blocks, near_values, preferred_element_type=jnp.float32
    )
    grad_far_weights = jnp.einsum(
        "bqnhe,nhbke->bnhqk", grad_blocks, far_values, preferred_element_type=jnp.float32
    )
    grad_weights = jnp.concatenate([grad_near_weights, grad_far_weights], -1)
    row_dot = jnp.sum(weights_full * grad_weights, -1, keepdims=True)
    grad_scores = (weights_full * (grad_weights - row_dot)).astype(jnp.bfloat16)
    grad_near, grad_far = (grad_scores[..., :span], grad_scores[..., span:])
    grad_queries = score_scale * (
        jnp.einsum("bnhqt,btnhe->bqnhe", grad_near, near_keys, preferred_element_type=jnp.float32)
        + jnp.einsum("bnhqk,nhbke->bqnhe", grad_far, far_keys, preferred_element_type=jnp.float32)
    )
    near_key_grad = score_scale * jnp.einsum(
        "bnhqt,bqnhe->btnhe", grad_near, query_blocks, preferred_element_type=jnp.float32
    )
    far_key_grad = score_scale * jnp.einsum(
        "bnhqk,bqnhe->nhbke", grad_far, query_blocks, preferred_element_type=jnp.float32
    )
    near_value_grad = jnp.einsum(
        "bnhqt,bqnhe->btnhe",
        softmax_low[..., :span],
        grad_blocks,
        preferred_element_type=jnp.float32,
    )
    far_value_grad = jnp.einsum(
        "bnhqk,bqnhe->nhbke",
        softmax_low[..., span:],
        grad_blocks,
        preferred_element_type=jnp.float32,
    )
    total_rows = key_rows.shape[0]
    key_grad = spread_back(
        near_key_grad, far_key_grad, flat_index, seq_start, seq_first, total_rows
    )
    value_grad = spread_back(
        near_value_grad, far_value_grad, flat_index, seq_start, seq_first, total_rows
    )
    return (grad_queries.reshape(queries.shape), key_grad, value_grad)


def forward_pass(hidden, params, chosen_now, query_mask, seq_start, seq_first, finish):
    (
        ln1_gain,
        ln1_shift,
        w_qkv,
        b_qv,
        w_out,
        b_out,
        ln2_gain,
        ln2_shift,
        w_fc,
        b_fc,
        w_proj,
        b_proj,
    ) = params
    hidden_wide = hidden.astype(jnp.float32)
    normed_all = gather_rows(layer_norm(hidden_wide, ln1_gain, ln1_shift).astype(jnp.bfloat16))
    projected = jnp.einsum("pnd,jdc->jpnc", normed_all, w_qkv, preferred_element_type=jnp.float32)
    queries = (projected[0] + b_qv[0]).astype(jnp.bfloat16)
    key_rows, value_rows = (
        lax.all_gather(projected[1].astype(jnp.bfloat16), "seq", axis=0, tiled=True),
        lax.all_gather((projected[2] + b_qv[1]).astype(jnp.bfloat16), "seq", axis=0, tiled=True),
    )
    attended, log_total = attend(queries, key_rows, value_rows, chosen_now, seq_start, seq_first)
    mixed_rows = (attended * query_mask[:, :, None]).astype(jnp.bfloat16)
    middle = hidden_wide + scatter_product(mixed_rows, w_out, "pnc,cd->pnd") + b_out
    normed_mlp = gather_rows(layer_norm(middle, ln2_gain, ln2_shift).astype(jnp.bfloat16))
    pre_active = (
        jnp.einsum("pnd,df->pnf", normed_mlp, w_fc, preferred_element_type=jnp.float32) + b_fc
    )
    active = gelu_tanh(pre_active).astype(jnp.bfloat16)
    if not finish:
        return (
            normed_all,
            queries,
            key_rows,
            value_rows,
            log_total,
            mixed_rows,
            middle,
            normed_mlp,
            pre_active,
            active,
        )
    output = (middle + scatter_product(active, w_proj, "pnf,fd->pnd") + b_proj).astype(jnp.bfloat16)
    return (output, (key_rows, value_rows))


def backward_pass(hidden, upstream, params, chosen_now, query_mask, seq_start, seq_first):
    (
        ln1_gain,
        ln1_shift,
        w_qkv,
        b_qv,
        w_out,
        b_out,
        ln2_gain,
        ln2_shift,
        w_fc,
        b_fc,
        w_proj,
        b_proj,
    ) = params
    (
        normed_all,
        queries,
        key_rows,
        value_rows,
        log_total,
        mixed_rows,
        middle,
        normed_mlp,
        pre_active,
        active,
    ) = forward_pass(hidden, params, chosen_now, query_mask, seq_start, seq_first, False)
    upstream_all = gather_rows(upstream)
    grad_w_proj = jnp.einsum(
        "pnf,pnd->fd", active, upstream_all, preferred_element_type=jnp.float32
    )
    grad_b_proj = jnp.sum(upstream.astype(jnp.float32), axis=(0, 1))
    grad_active = jnp.einsum(
        "pnd,fd->pnf", upstream_all, w_proj, preferred_element_type=jnp.float32
    )
    unused_value, gelu_pull = jax.vjp(gelu_tanh, pre_active)
    grad_pre = gelu_pull(grad_active)[0].astype(jnp.bfloat16)
    grad_w_fc = jnp.einsum("pnd,pnf->df", normed_mlp, grad_pre, preferred_element_type=jnp.float32)
    grad_b_fc = jnp.sum(grad_pre.astype(jnp.float32), axis=(0, 1))
    grad_normed_mlp = scatter_product(grad_pre, w_fc, "pnf,df->pnd")
    unused_norm, second_pull = jax.vjp(layer_norm, middle, ln2_gain, ln2_shift)
    grad_mid_norm, grad_ln2_gain, grad_ln2_shift = second_pull(grad_normed_mlp)
    grad_middle = upstream.astype(jnp.float32) + grad_mid_norm
    grad_branch = grad_middle.astype(jnp.bfloat16)
    grad_b_out = jnp.sum(grad_branch.astype(jnp.float32), axis=(0, 1))
    branch_all = gather_rows(grad_branch)
    grad_w_out = jnp.einsum(
        "pnc,pnd->cd", mixed_rows, branch_all, preferred_element_type=jnp.float32
    )
    grad_mixed = jnp.einsum(
        "pnd,cd->pnc", branch_all, w_out, preferred_element_type=jnp.float32
    ).astype(jnp.bfloat16) * query_mask[:, :, None].astype(jnp.bfloat16)
    grad_queries, key_grad_all, value_grad_all = attend_back(
        queries, key_rows, value_rows, chosen_now, seq_start, seq_first, log_total, grad_mixed
    )
    key_grad, value_grad = (
        lax.psum_scatter(
            key_grad_all.astype(jnp.bfloat16), "seq", scatter_dimension=0, tiled=True
        ).astype(jnp.float32),
        lax.psum_scatter(
            value_grad_all.astype(jnp.bfloat16), "seq", scatter_dimension=0, tiled=True
        ).astype(jnp.float32),
    )
    grad_project = jnp.stack(
        [
            grad_queries.astype(jnp.bfloat16),
            key_grad.astype(jnp.bfloat16),
            value_grad.astype(jnp.bfloat16),
        ],
        2,
    )
    grad_w_qkv = jnp.einsum(
        "pnd,pnjc->jdc", normed_all, grad_project, preferred_element_type=jnp.float32
    )
    grad_b_qv = jnp.sum(grad_project[:, :, 0::2].astype(jnp.float32), axis=(0, 1))
    grad_normed = scatter_product(grad_project, w_qkv, "pnjc,jdc->pnd")
    unused_first, first_pull = jax.vjp(layer_norm, hidden.astype(jnp.float32), ln1_gain, ln1_shift)
    grad_in_norm, grad_ln1_gain, grad_ln1_shift = first_pull(grad_normed)
    grad_hidden = (grad_middle + grad_in_norm).astype(jnp.bfloat16)
    block_grads = (
        grad_ln1_gain,
        grad_ln1_shift,
        grad_w_qkv,
        grad_b_qv,
        grad_w_out,
        grad_b_out,
        grad_ln2_gain,
        grad_ln2_shift,
        grad_w_fc,
        grad_b_fc,
        grad_w_proj,
        grad_b_proj,
    )
    return (grad_hidden, block_grads)


def on_device(
    inputs,
    cotangent,
    lengths,
    chosen,
    ln1_gain,
    ln1_shift,
    w_qkv,
    b_qv,
    w_out,
    b_out,
    ln2_gain,
    ln2_shift,
    w_fc,
    b_fc,
    w_proj,
    b_proj,
):
    params = tuple(
        (
            weight_array[0]
            for weight_array in (
                ln1_gain,
                ln1_shift,
                w_qkv,
                b_qv,
                w_out,
                b_out,
                ln2_gain,
                ln2_shift,
                w_fc,
                b_fc,
                w_proj,
                b_proj,
            )
        )
    )
    section_index = lax.axis_index("section")
    section_count = lax.axis_size("section")
    seq_index = lax.axis_index("seq")
    tensor_index = lax.axis_index("tensor")
    tensor_count = lax.axis_size("tensor")
    micro_count, rows_local, buckets, feature_width = inputs.shape
    length_local = rows_local * tensor_count
    heads_width = w_qkv.shape[-1]
    seq_start = seq_index * length_local
    seq_first = seq_index == 0
    positions = seq_start + lax.broadcasted_iota(jnp.int32, (micro_count, length_local, buckets), 1)
    mask_all = (positions < lengths[:, None, :]).astype(jnp.float32)
    mask_rows = lax.dynamic_slice_in_dim(mask_all, tensor_index * rows_local, rows_local, 1)
    step_count = micro_count + section_count - 1
    chosen_section = chosen[0]
    received = jnp.zeros((rows_local, buckets, feature_width), jnp.bfloat16)
    stored = jnp.zeros((micro_count, rows_local, buckets, feature_width), jnp.bfloat16)
    outputs = jnp.zeros_like(stored)
    for step_index in range(step_count):
        micro_index = step_index - section_index
        running = (micro_index >= 0) & (micro_index < micro_count)
        slot_index = jnp.clip(micro_index, 0, micro_count - 1)
        block_in = jnp.where(
            section_index == 0, lax.dynamic_index_in_dim(inputs, slot_index, 0, False), received
        )
        chosen_now = lax.dynamic_index_in_dim(chosen_section, slot_index, 0, False)
        query_mask = lax.dynamic_index_in_dim(mask_all, slot_index, 0, False)
        result, key_pair = forward_pass(
            block_in, params, chosen_now, query_mask, seq_start, seq_first, True
        )
        stored = jnp.where(
            running, lax.dynamic_update_index_in_dim(stored, block_in, slot_index, 0), stored
        )
        outputs = jnp.where(
            running, lax.dynamic_update_index_in_dim(outputs, result, slot_index, 0), outputs
        )
        received = from_behind(result, "section", 1)
    back_received = jnp.zeros((rows_local, buckets, feature_width), jnp.bfloat16)
    in_grads = jnp.zeros_like(stored)
    totals = None
    for step_index in range(step_count):
        micro_index = step_index - (section_count - 1 - section_index)
        running = (micro_index >= 0) & (micro_index < micro_count)
        slot_index = jnp.clip(micro_index, 0, micro_count - 1)
        chosen_now = lax.dynamic_index_in_dim(chosen_section, slot_index, 0, False)
        query_mask = lax.dynamic_index_in_dim(mask_all, slot_index, 0, False)
        local_mask = lax.dynamic_index_in_dim(mask_rows, slot_index, 0, False)
        top_grad = (
            lax.dynamic_index_in_dim(cotangent, slot_index, 0, False).astype(jnp.float32)
            * local_mask[:, :, None]
        ).astype(jnp.bfloat16)
        upstream = jnp.where(section_index == section_count - 1, top_grad, back_received)
        hidden = lax.dynamic_index_in_dim(stored, slot_index, 0, False)
        grad_hidden, block_grads = backward_pass(
            hidden, upstream, params, chosen_now, query_mask, seq_start, seq_first
        )
        block_grads = tuple(
            (jnp.where(running, grad_part, jnp.zeros_like(grad_part)) for grad_part in block_grads)
        )
        totals = (
            block_grads
            if step_index == 0
            else tuple(
                (total_part + grad_part for total_part, grad_part in zip(totals, block_grads))
            )
        )
        in_grads = jnp.where(
            running, lax.dynamic_update_index_in_dim(in_grads, grad_hidden, slot_index, 0), in_grads
        )
        back_received = from_behind(grad_hidden, "section", -1)
    (
        sum_ln1_gain,
        sum_ln1_shift,
        sum_w_qkv,
        sum_b_qv,
        sum_w_out,
        sum_b_out,
        sum_ln2_gain,
        sum_ln2_shift,
        sum_w_fc,
        sum_b_fc,
        sum_w_proj,
        sum_b_proj,
    ) = totals
    part_qkv, part_out, part_fc, part_proj = (
        lax.psum_scatter(
            sum_w_qkv.astype(jnp.bfloat16), "seq", scatter_dimension=1, tiled=True
        ).astype(jnp.float32),
        lax.psum_scatter(
            sum_w_out.astype(jnp.bfloat16), "seq", scatter_dimension=1, tiled=True
        ).astype(jnp.float32),
        lax.psum_scatter(
            sum_w_fc.astype(jnp.bfloat16), "seq", scatter_dimension=0, tiled=True
        ).astype(jnp.float32),
        lax.psum_scatter(
            sum_w_proj.astype(jnp.bfloat16), "seq", scatter_dimension=1, tiled=True
        ).astype(jnp.float32),
    )
    bias_qv = lax.dynamic_update_slice_in_dim(
        jnp.zeros((2, feature_width), jnp.float32), sum_b_qv, tensor_index * heads_width, 1
    )
    units_local = sum_b_fc.shape[0]
    bias_fc = lax.dynamic_update_slice_in_dim(
        jnp.zeros((units_local * tensor_count,), jnp.float32),
        sum_b_fc,
        tensor_index * units_local,
        0,
    )
    small_sums = lax.psum(
        (
            sum_ln1_gain,
            sum_ln1_shift,
            bias_qv,
            sum_b_out,
            sum_ln2_gain,
            sum_ln2_shift,
            bias_fc,
            sum_b_proj,
        ),
        ("seq", "tensor"),
    )
    return (
        outputs[None],
        in_grads[None],
        small_sums[0][None],
        small_sums[1][None],
        part_qkv[None],
        small_sums[2][None],
        part_out[None],
        small_sums[3][None],
        small_sums[4][None],
        small_sums[5][None],
        part_fc[None],
        small_sums[6][None],
        part_proj[None],
        small_sums[7][None],
    )


STREAMS = 4
NRM, NMLP, UPS, BRN, ACT, GPRE, MIX, DQKV = range(8)
F32 = jnp.float32
LOW = jnp.bfloat16
MESH_ID = pl.DeviceIdType.MESH


def dot_nn(left, right):
    return lax.dot_general(left, right, (((1,), (0,)), ((), ())), preferred_element_type=F32)


def dot_nt(left, right):
    return lax.dot_general(left, right, (((1,), (1,)), ((), ())), preferred_element_type=F32)


def dot_tn(left, right):
    return lax.dot_general(left, right, (((0,), (0,)), ((), ())), preferred_element_type=F32)


def standard(rows):
    centred = rows - jnp.mean(rows, axis=-1, keepdims=True)
    scale = lax.rsqrt(jnp.mean(centred * centred, axis=-1, keepdims=True) + NORM_EPS)
    return centred * scale, scale


def standard_back(grad, xhat, scale):
    inner = jnp.mean(grad * xhat, axis=-1, keepdims=True)
    return scale * (grad - jnp.mean(grad, axis=-1, keepdims=True) - xhat * inner)


def column_sum(rows):
    return jnp.sum(rows.astype(F32), axis=0, keepdims=True)


def relay_kernel(names, *refs):
    r = types.SimpleNamespace(**dict(zip(names, refs)))
    a, c, t = (lax.axis_index(name) for name in ("section", "seq", "tensor"))
    lines = lax.axis_size("section")
    chips = lax.axis_size("tensor")
    rows, buckets, width = r.inputs.shape[1:]
    half_width = width // 2
    local = rows * chips
    total = 2 * local
    stream_rows = local // STREAMS
    head_width = r.wo_in.shape[0]
    heads = head_width // HDIM
    blocks = local // QB
    units = r.wp_in.shape[0]
    scale = HDIM ** (-0.5)
    streams = range(STREAMS)

    def remote(src, dst, send, recv, **target):
        return pltpu.make_async_remote_copy(
            src_ref=src,
            dst_ref=dst,
            send_sem=send,
            recv_sem=recv,
            device_id=target,
            device_id_type=MESH_ID,
        )

    def drain(ref, sem):
        pltpu.make_async_copy(ref, ref, sem).wait()

    def row_block(index, size):
        return pl.ds(pl.multiple_of(index * size, size), size)

    near_chip = t + 1 - 2 * (t % 2)
    over_chip = (t + 2) % 4
    across_chip = 3 - t
    middle_chip = (t == 1) | (t == 2)
    end_chip = (t == 0) | (t == 3)
    owned = stream_rows // 2
    mine = row_block(t - 1, owned)
    my_half = row_block(c, local)

    barrier = pltpu.get_barrier_semaphore()
    for core in range(2):
        for step in range(1, chips):
            there = {"tensor": (t + step) % chips, "seq": core}
            pl.semaphore_signal(barrier, inc=1, device_id=there, device_id_type=MESH_ID)
        for step in range(1, lines):
            there = {"section": (a + step) % lines, "seq": core}
            pl.semaphore_signal(barrier, inc=1, device_id=there, device_id_type=MESH_ID)
    for step in range(1, lines):
        there = {"section": (a + step) % lines, "tensor": near_chip}
        pl.semaphore_signal(barrier, inc=1, device_id=there, device_id_type=MESH_ID)
    pl.semaphore_signal(barrier, inc=1, device_id={"seq": 1 - c}, device_id_type=MESH_ID)
    pl.semaphore_wait(barrier, 2 * (chips - 1) + 3 * (lines - 1) + 1)

    def beside(s):
        return s + 1 - 2 * (s % 2)

    def above(s):
        return (s + 2) % 4

    def store(p):
        return (r.wq, r.wo, r.wf, r.wp)[p]

    def source(p):
        return (r.wq_in, r.wo_in, r.wf_in, r.wp_in)[p]

    def height(p):
        return source(p).shape[0]

    def core_half(p, s, core):
        return store(p).at[s, row_block(core, height(p) // 2)]

    def first_hop(p, s, neighbour, which):
        return remote(
            source(p).at[row_block(c, height(p) // 2)],
            core_half(p, s, c),
            r.w_first_s.at[p, which],
            r.w_first_r.at[s, p],
            section=neighbour,
        )

    def second_hop(p, s, which):
        view = store(p).at[s, row_block(2 * c + which, height(p) // 4)]
        return remote(
            view, view, r.w_second_s.at[s, p], r.w_second_r.at[s, p, which], section=3 - s
        )

    def core_hop(p, s, core):
        view = core_half(p, s, core)
        return remote(view, view, r.w_core_s.at[s, p], r.w_core_r.at[s, p], seq=1 - c)

    def own_copy(p):
        return pltpu.make_async_copy(source(p), store(p).at[a], r.w_own.at[p])

    def pass_on(s, p, which):
        line = (beside(s), above(s))[which]

        @pl.when(a == line)
        def _():
            first_hop(p, s, line, which).wait_recv()
            second_hop(p, s, which).start()
            core_hop(p, s, c).start()

    def pass_all(s, pieces):
        for p in pieces:
            for which in range(2):
                pass_on(s, p, which)

    def pass_far(s, p):
        @pl.when(a == 3 - s)
        def _():
            second_hop(p, s, 0).wait_recv()
            second_hop(p, s, 1).wait_recv()
            core_hop(p, s, c).start()

    def need(s, p):
        @pl.when(s == 0)
        def _():
            if p < 2:
                pass_all(0, (p,))
            pass_far(0, p)

        @pl.when(a == s)
        def _():
            own_copy(p).wait()

        @pl.when(a != s)
        def _():
            core_hop(p, s, 1 - c).wait_recv()

    def small_copy(step, line, slot):
        return remote(
            r.small_own, r.small.at[slot], r.small_s.at[step], r.small_r.at[slot], section=line
        )

    def count_copy(step, line, slot):
        return remote(
            r.count_own.at[line],
            r.count.at[slot],
            r.count_s.at[step],
            r.count_r.at[slot],
            section=line,
        )

    singles = (r.ln1_gain, r.ln1_shift, r.ln2_gain, r.ln2_shift, r.b_out, r.b_proj)
    for place, single in enumerate(singles):
        r.small_own[place : place + 1] = single[...]
    r.small_own[6:7, :units] = r.b_fc[...]
    r.small_own[7:8, :head_width] = r.b_qv[0:1]
    r.small_own[7:8, half_width : half_width + head_width] = r.b_qv[1:2]
    for step in range(1, lines):
        small_copy(step - 1, (a + step) % lines, a).start()
    for p in range(4):
        for which, line in enumerate((beside(a), above(a))):
            first_hop(p, a, line, which).start()
    for p in range(4):
        own_copy(p).start()
    r.small[a] = r.small_own[...]

    def place_of(index):
        inside = index % local
        stream, left = inside // stream_rows, inside % stream_rows
        first = (index // local) * local + (left // owned) * (local // 2)
        return first + stream * owned + left % owned

    def iota(shape, dimension):
        return lax.broadcasted_iota(jnp.int32, shape, dimension)

    square = jnp.where(iota((KSEL, KSEL), 0) == iota((KSEL, KSEL), 1), 1.0, 0.0).astype(LOW)
    position = place_of(iota((KSEL, total), 1)).astype(F32)
    for pair in range(lines * heads):
        line, head = pair // heads, pair % heads
        columns = dot_nt(square, r.chosen[pair].astype(F32).astype(LOW))
        for block in range(blocks):
            pick = head * blocks + block
            r.count_own[line, pick : pick + 1, :] = jnp.sum(
                jnp.where(columns[:, block : block + 1] == position, 1.0, 0.0),
                axis=0,
                keepdims=True,
            )
    for step in range(1, lines):
        count_copy(step - 1, (a + step) % lines, a).start()
    r.count[a] = r.count_own[a]

    NEAR, OVER, ACROSS = range(3)

    def gather(buffer, s, kind, j, owner, target, slot):
        view = buffer.at[s, j, row_block(owner - 1, owned)]
        return remote(
            view, view, r.ag_s.at[kind, j, slot], r.ag_r.at[kind, j, slot], tensor=target
        )

    def used_before(s, kind):
        return s > 0 if kind < 2 else s < lines - 1

    def gather_start(buffer, s, kind, j):
        @pl.when(used_before(s, kind))
        def _():
            gather_sent(buffer, s, kind, j)

        gather(buffer, s, kind, j, t, over_chip, OVER).start()
        gather(buffer, s, kind, j, t, across_chip, ACROSS).start()
        gather(buffer, s, kind, j, t, near_chip, NEAR).start()

    def gather_wait(buffer, s, kind, j):
        @pl.when(middle_chip)
        def _():
            gather(buffer, s, kind, j, across_chip, across_chip, ACROSS).wait_recv()

        @pl.when(end_chip)
        def _():
            gather(buffer, s, kind, j, near_chip, near_chip, NEAR).wait_recv()
            gather(buffer, s, kind, j, over_chip, over_chip, OVER).wait_recv()

    def gather_sent(buffer, s, kind, j):
        gather(buffer, s, kind, j, t, over_chip, OVER).wait_send()
        gather(buffer, s, kind, j, t, across_chip, ACROSS).wait_send()
        gather(buffer, s, kind, j, t, near_chip, NEAR).wait_send()

    def scatter(s, kind, j, owner, slot):
        return remote(
            r.part.at[kind, j, row_block(owner - 1, owned)],
            r.arrived.at[s, kind, j, slot],
            r.rs_s.at[kind, j, slot],
            r.rs_r.at[kind, j, slot],
            tensor=owner,
        )

    def scatter_start(s, kind, j, product):
        @pl.when(used_before(s, kind))
        def _():
            scatter_sent(s, kind, j)

        r.part[kind, j] = product.astype(LOW)

        @pl.when(end_chip)
        def _():
            scatter(s, kind, j, over_chip, OVER).start()
            scatter(s, kind, j, near_chip, NEAR).start()

        @pl.when(middle_chip)
        def _():
            scatter(s, kind, j, across_chip, ACROSS).start()

    def scatter_sum(s, kind, j):
        result = r.part[kind, j, mine].astype(F32)
        for slot in (NEAR, ACROSS, OVER):
            scatter(s, kind, j, t, slot).wait_recv()
            result = result + r.arrived[s, kind, j, slot].astype(F32)
        return result

    def scatter_sent(s, kind, j):
        @pl.when(end_chip)
        def _():
            scatter(s, kind, j, over_chip, OVER).wait_send()
            scatter(s, kind, j, near_chip, NEAR).wait_send()

        @pl.when(middle_chip)
        def _():
            scatter(s, kind, j, across_chip, ACROSS).wait_send()

    own_rows = (r.nrm, r.nmlp, r.ups, r.brn, r.act, r.gpre, r.mix, r.dqkv)
    all_rows = (
        r.all_nrm,
        r.all_nmlp,
        r.all_ups,
        r.all_brn,
        r.all_act,
        r.all_gpre,
        r.all_mix,
        r.all_dqkv,
    )

    def rows_copy(index, s, same, stays=False):
        core = c if same else 1 - c
        src = own_rows[index].at[s]
        dst = all_rows[index].at[a, c]
        if index <= BRN:
            src = src.at[:, :, row_block(core, half_width)]
        recv = r.rows_r.at[index]
        if stays:
            return pltpu.make_async_copy(src, dst, recv)
        if same:
            return remote(src, dst, r.rows_s.at[index, s, 0], recv, section=s)
        return remote(src, dst, r.rows_s.at[index, s, 1], recv, section=s, seq=1 - c)

    def rows_start(index, s):
        @pl.when(a == s)
        def _():
            rows_copy(index, s, True, True).start()

        @pl.when(a != s)
        def _():
            rows_copy(index, s, True).start()

        if index <= BRN:
            rows_copy(index, s, False).start()

    def forward_rows(s):
        for index in (NRM, MIX, NMLP, ACT):
            rows_start(index, s)

    def rows_sent(index, s):
        @pl.when(a != s)
        def _():
            rows_copy(index, s, True).wait_send()

        if index <= BRN:
            rows_copy(index, s, False).wait_send()

    def share_copy(index, core):
        view = all_rows[index].at[:, core]
        return remote(view, view, r.share_s.at[index - ACT], r.share_r.at[index - ACT], seq=1 - c)

    def share(index):
        drain(all_rows[index].at[:, c], r.rows_r.at[index])
        share_copy(index, c).start()

    def norm_copy(s):
        return remote(
            r.norm_part.at[s], r.norm_all.at[a], r.norm_s.at[s], r.norm_r, section=s
        )

    def norm_start(s):
        @pl.when(a == s)
        def _():
            pltpu.make_async_copy(r.norm_part.at[s], r.norm_all.at[a], r.norm_r).start()

        @pl.when(a != s)
        def _():
            norm_copy(s).start()

    def home_copy(what, s, chip):
        src, dst, send, recv = what
        return remote(
            src.at[s, chip % 2],
            dst.at[a],
            send.at[s, chip % 2],
            recv,
            section=s,
            tensor=chip,
        )

    def home_start(what, s):
        src, dst, send, recv = what

        @pl.when(middle_chip & (a == s))
        def _():
            pltpu.make_async_copy(src.at[s, t % 2], dst.at[a], recv).start()

        @pl.when(middle_chip & (a != s))
        def _():
            home_copy(what, s, t).start()

        @pl.when(middle_chip)
        def _():
            home_copy(what, s, near_chip).start()

    def home_sent(what, s):
        @pl.when(middle_chip & (a != s))
        def _():
            home_copy(what, s, t).wait_send()

        @pl.when(middle_chip)
        def _():
            home_copy(what, s, near_chip).wait_send()

    out_home = (r.out_low, r.acts, r.out_s, r.out_r)
    grad_home = (r.grad_low, r.grads, r.grad_s, r.grad_r)

    length = r.lengths[a // buckets, a % buckets]
    key = place_of(iota((stream_rows, total), 1))
    for j in streams:
        query = place_of(c * local + j * stream_rows + iota((stream_rows, total), 0))
        r.near[j] = jnp.where((query >= key) & (query - key < WIN), 1.0, 0.0)
    key_row = place_of(iota((1, total), 1))

    def row_mask(place):
        return jnp.where(place < length, 1.0, 0.0)

    def multiplicity(s, j, head):
        far = []
        for block in range(blocks):
            pick = head * blocks + block
            limit = (c * blocks + block) * QB - WIN
            counted = jnp.where(key_row <= limit, r.count[s, pick : pick + 1, :], 0.0)
            far.append(jnp.broadcast_to(counted, (stream_rows // blocks, total)))
        return r.near[j] + jnp.concatenate(far, axis=0)

    def head_cols(head):
        return slice(head * HDIM, (head + 1) * HDIM)

    def kv_copy(s):
        view = r.kv.at[s, :, 0:local]
        return remote(view, view, r.kv_s.at[s], r.kv_r.at[s], seq=1 - c)

    def dkv_copy(s):
        return remote(r.dkv_out.at[s], r.dkv_in.at[s], r.dkv_s.at[s], r.dkv_r.at[s], seq=1 - c)

    def own_sequence(ref):
        both = ref[a // buckets].astype(F32)
        picked = both[:, 0, :]
        for bucket in range(1, buckets):
            picked = jnp.where(a % buckets == bucket, both[:, bucket, :], picked)
        return picked

    def own_part(j):
        chip, first = (j * owned) // rows, (j * owned) % rows
        return chip, slice(first, first + owned)

    def first_copy():
        return remote(r.first_out, r.first_in, r.first_s, r.first_r, tensor=near_chip)

    own_place = c * local + t * rows + iota((rows, 1), 0)
    r.first_out[0] = own_sequence(r.inputs).astype(LOW)
    r.first_out[1] = (own_sequence(r.cotangent) * row_mask(own_place)).astype(LOW)
    r.norm_part[...] = jnp.zeros_like(r.norm_part)

    @pl.when(c == 0)
    def _():
        r.kv[:, :, local:total] = jnp.zeros((lines, 2, local, head_width), LOW)


    @pl.when(end_chip)
    def _():
        first_copy().start()

    @pl.when(middle_chip)
    def _():
        first_copy().wait_recv()
        for which in range(2):
            here, beside_it = r.first_out[which].astype(F32), r.first_in[which].astype(F32)
            lower = jnp.where(t % 2 == 0, here, beside_it)
            upper = jnp.where(t % 2 == 0, beside_it, here)
            for j in streams:
                chip, part = own_part(j)
                own_block = (lower, upper)[chip][part]
                if which == 0:
                    r.hidden[j] = own_block
                else:
                    r.upstream[j] = own_block.astype(LOW)

    def on_owner(stage):
        def run(s, j):
            @pl.when(middle_chip)
            def _():
                stage(s, j)

        return run

    def keep_rows(target, s, j, result):
        chip, part = own_part(j)
        target[s, chip, part] = result

    @on_owner
    def enter(s, j):
        xhat, inverse = standard(r.hidden[j])
        r.xhat1[s, j] = xhat
        r.inv1[s, j] = jnp.broadcast_to(inverse, (owned, 128))
        r.nrm[s, j, mine] = (xhat * r.small[s, 0:1] + r.small[s, 1:2]).astype(LOW)
        gather_start(r.nrm, s, 0, j)

    def project(s, j):
        gather_wait(r.nrm, s, 0, j)
        normed = r.nrm[s, j]
        place = row_block(c * STREAMS + j, stream_rows)
        bias_v = r.small[s, 7:8, half_width : half_width + head_width]
        key_rows = dot_nt(normed, r.wq[s, head_width : 2 * head_width])
        value_rows = dot_nt(normed, r.wq[s, 2 * head_width : 3 * head_width]) + bias_v
        r.kv[s, 0, place] = key_rows.astype(LOW)
        r.kv[s, 1, place] = value_rows.astype(LOW)

    def ask(s, j):
        queries = dot_nt(r.nrm[s, j], r.wq[s, 0:head_width]) + r.small[s, 7:8, :head_width]
        r.qry[s, j] = queries.astype(LOW)

    def attend_line(s, j):
        mixed = []
        for head in range(heads):
            cols = head_cols(head)
            times = multiplicity(s, j, head)
            scores = scale * dot_nt(r.qry[s, j, :, cols], r.kv[s, 0, :, cols])
            scores = jnp.where(times > 0.0, scores, MASKED)
            top = jnp.max(scores, axis=-1, keepdims=True)
            terms = times * jnp.exp(scores - top)
            weights = terms / jnp.sum(terms, axis=-1, keepdims=True)
            r.soft[s, j, head] = weights
            mixed.append(dot_nn(weights.astype(LOW), r.kv[s, 1, :, cols]))
        mask = row_mask(place_of(c * local + j * stream_rows + iota((stream_rows, 1), 0)))
        r.mix[s, j] = (jnp.concatenate(mixed, axis=-1) * mask).astype(LOW)

    def leave_attention(s, j):
        scatter_start(s, 0, j, dot_nn(r.mix[s, j], r.wo[s]))

    @on_owner
    def between(s, j):
        middle = r.hidden[j] + scatter_sum(s, 0, j) + r.small[s, 4:5]
        r.middle[j] = middle
        xhat, inverse = standard(middle)
        r.xhat2[s, j] = xhat
        r.inv2[s, j] = jnp.broadcast_to(inverse, (owned, 128))
        r.nmlp[s, j, mine] = (xhat * r.small[s, 2:3] + r.small[s, 3:4]).astype(LOW)
        gather_start(r.nmlp, s, 1, j)

    def feed(s, j):
        gather_wait(r.nmlp, s, 1, j)
        before = dot_nn(r.nmlp[s, j], r.wf[s]) + r.small[s, 6:7, :units]
        bend = jnp.tanh(0.7978845608028654 * (before + 0.044715 * before * before * before))
        r.act[s, j] = (0.5 * before * (1.0 + bend)).astype(LOW)
        r.slope[s, j] = 0.5 * (1.0 + bend) + 0.5 * before * (1.0 - bend * bend) * (
            0.7978845608028654 * (1.0 + 3 * 0.044715 * before * before)
        )


    def leave_feed(s, j):
        scatter_start(s, 1, j, dot_nn(r.act[s, j], r.wp[s]))

    @on_owner
    def finish(s, j):
        result = r.middle[j] + scatter_sum(s, 1, j) + r.small[s, 5:6]
        keep_rows(r.out_low, s, j, result.astype(LOW))
        r.hidden[j] = result.astype(LOW).astype(F32)

    def small_ready(s):
        @pl.when(a != s)
        def _():
            small_copy(0, a, s).wait_recv()

    small_ready(0)
    for j in streams:
        enter(0, j)

    def forward(s, _):
        need(s, 0)
        for j in streams:
            project(s, j)

        @pl.when(c == 0)
        def _():
            kv_copy(s).start()

        for j in streams:
            ask(s, j)

        @pl.when(a != s)
        def _():
            count_copy(0, a, s).wait_recv()

        @pl.when(c == 1)
        def _():
            kv_copy(s).wait_recv()

        for j in streams:
            attend_line(s, j)
            if j == 0:
                need(s, 1)
            leave_attention(s, j)

        @pl.when(s == 0)
        def _():
            pass_all(0, (2,))
            for later in range(1, lines):
                pass_all(later, (0, 1, 2))

        @pl.when(s == 1)
        def _():
            pass_far(1, 2)
            pass_far(1, 3)
            for later in range(2, lines):
                for p in range(4):
                    pass_far(later, p)

        for j in streams:
            between(s, j)
        @pl.when(s == 0)
        def _():
            for later in range(lines):
                pass_all(later, (3,))

        need(s, 2)
        for j in streams:
            feed(s, j)
            if j == 0:
                need(s, 3)
            leave_feed(s, j)


        @pl.when(s >= 2)
        def _():
            forward_rows(s - 2)


        @pl.when(s + 1 < lines)
        def _():
            small_ready(s + 1)

        for j in streams:
            finish(s, j)

            @pl.when(s + 1 < lines)
            def _():
                enter(s + 1, j)

        home_start(out_home, s)

        @pl.when(s == 0)
        def _():
            pass_far(1, 0)
            pass_far(1, 1)

        return 0

    lax.fori_loop(0, lines, forward, 0)

    @on_owner
    def turn(s, j):
        upstream = r.upstream[j]
        r.ups[s, j, mine] = upstream
        gather_start(r.ups, s, 2, j)
        r.norm_part[s, 5:6] += column_sum(upstream)

    def feed_back(s, j):
        gather_wait(r.ups, s, 2, j)
        grad_pre = (dot_nt(r.ups[s, j], r.wp[s]) * r.slope[s, j]).astype(LOW)
        r.gpre[s, j] = grad_pre
        scatter_start(s, 2, j, dot_nt(grad_pre, r.wf[s]))
        r.norm_part[s, 6:7, :units] += column_sum(grad_pre)

    @on_owner
    def between_back(s, j):
        grad = scatter_sum(s, 2, j)
        xhat = r.xhat2[s, j]
        upstream = r.upstream[j].astype(F32)
        grad_middle = upstream + standard_back(
            grad * r.small[s, 2:3], xhat, r.inv2[s, j, :, 0:1]
        )
        r.middle[j] = grad_middle
        branch = grad_middle.astype(LOW)
        r.brn[s, j, mine] = branch
        gather_start(r.brn, s, 3, j)
        r.norm_part[s, 2:3] += column_sum(grad * xhat)
        r.norm_part[s, 3:4] += column_sum(grad)
        r.norm_part[s, 4:5] += column_sum(branch)

    def mixed_back(s, j):
        gather_wait(r.brn, s, 3, j)
        place = place_of(c * local + j * stream_rows + iota((stream_rows, 1), 0))
        r.gmix[j] = (dot_nt(r.brn[s, j], r.wo[s]) * row_mask(place)).astype(LOW)

    def attend_line_back(s, j):
        grad_q, grad_k, grad_v = [], [], []
        for head in range(heads):
            cols = head_cols(head)
            weights = r.soft[s, j, head]
            grad_head = r.gmix[j, :, cols]
            grad_weights = dot_nt(grad_head, r.kv[s, 1, :, cols])
            inner = jnp.sum(weights * grad_weights, axis=-1, keepdims=True)
            grad_scores = (weights * (grad_weights - inner)).astype(LOW)
            grad_k.append(scale * dot_tn(grad_scores, r.qry[s, j, :, cols]))
            grad_v.append(dot_tn(weights.astype(LOW), grad_head))
            grad_q.append(scale * dot_nn(grad_scores, r.kv[s, 0, :, cols]))
        for which, grad in enumerate((grad_k, grad_v)):
            grad = jnp.concatenate(grad, axis=-1)
            r.dkv_all[which] = grad if j == 0 else r.dkv_all[which] + grad
        grad_q = jnp.concatenate(grad_q, axis=-1).astype(LOW)
        r.dqkv[s, 0, j] = grad_q
        r.norm_part[s, 7:8, :head_width] += column_sum(grad_q)

    def join_keys(s):
        @pl.when(c == 1)
        def _():
            r.dkv_out[s] = r.dkv_all[:, 0:local].astype(LOW)
            dkv_copy(s).start()

        @pl.when(c == 0)
        def _():
            dkv_copy(s).wait_recv()
            r.dkv_all[:, 0:local] += r.dkv_in[s].astype(F32)

        for which in range(2):
            joined = r.dkv_all[which, my_half].astype(LOW)
            r.dqkv[s, 1 + which] = joined.reshape(r.dqkv.shape[2:])
            if which == 1:
                r.norm_part[s, 7:8, half_width : half_width + head_width] = column_sum(joined)

    def leave_back(s, j):
        product = dot_nn(r.dqkv[s, 0, j], r.wq[s, 0:head_width])
        for which in range(1, 3):
            weight = r.wq[s, which * head_width : (which + 1) * head_width]
            product = product + dot_nn(r.dqkv[s, which, j], weight)
        scatter_start(s, 3, j, product)

    @on_owner
    def finish_back(s, j):
        grad = scatter_sum(s, 3, j)
        xhat = r.xhat1[s, j]
        result = r.middle[j] + standard_back(
            grad * r.small[s, 0:1], xhat, r.inv1[s, j, :, 0:1]
        )
        r.upstream[j] = result.astype(LOW)
        keep_rows(r.grad_low, s, j, result.astype(LOW))
        r.norm_part[s, 0:1] += column_sum(grad * xhat)
        r.norm_part[s, 1:2] += column_sum(grad)

    for j in streams:
        turn(lines - 1, j)

    def backward(index, _):
        s = lines - 1 - index
        for j in streams:
            feed_back(s, j)
        rows_start(UPS, s)
        rows_start(GPRE, s)

        @pl.when(index < 2)
        def _():
            forward_rows(lines - 2 + index)

        @pl.when(index == lines - 1)
        def _():
            share(ACT)
            share(MIX)

        for j in streams:
            between_back(s, j)
        for j in streams:
            mixed_back(s, j)
            attend_line_back(s, j)
        join_keys(s)
        rows_start(BRN, s)
        for j in streams:
            leave_back(s, j)
        rows_start(DQKV, s)
        for j in streams:
            finish_back(s, j)

            @pl.when(s > 0)
            def _():
                turn(s - 1, j)

        norm_start(s)
        home_start(grad_home, s)
        return 0

    lax.fori_loop(0, lines, backward, 0)

    share(GPRE)
    share(DQKV)

    drain(r.norm_all, r.norm_r)
    slot = c * chips + t
    norm_sum = r.norm_all[0]
    for line in range(1, lines):
        norm_sum = norm_sum + r.norm_all[line]
    r.ends[slot] = norm_sum

    def ends_copy(step):
        core, chip = step // chips, step % chips
        view = r.ends.at[slot]
        return remote(
            view,
            view,
            r.ends_s.at[step - 1],
            r.ends_r,
            seq=(c + core) % 2,
            tensor=(t + chip) % chips,
        )

    for step in range(1, 2 * chips):
        ends_copy(step).start()

    for kind, buffer in enumerate((r.nrm, r.nmlp, r.ups, r.brn)):
        for j in streams:
            scatter_sent(0, kind, j)

            @pl.when(middle_chip)
            def _():
                gather_sent(buffer, 0, kind, j)

    for index in range(ACT):
        drain(all_rows[index], r.rows_r.at[index])
    for index in range(ACT, 8):
        share_copy(index, 1 - c).wait_recv()
        share_copy(index, c).wait_send()
    drain(r.acts, r.out_r)
    drain(r.grads, r.grad_r)
    drain(r.ends.at[0 : 2 * chips - 1], r.ends_r)
    for step in range(1, 2 * chips):
        ends_copy(step).wait_send()
    for step in range(1, lines):
        small_copy(step - 1, (a + step) % lines, a).wait_send()
        count_copy(step - 1, (a + step) % lines, a).wait_send()
    for p in range(4):
        for which, line in enumerate((beside(a), above(a))):
            first_hop(p, a, line, which).wait_send()

    @pl.when(end_chip)
    def _():
        first_copy().wait_send()

    def sent(s, _):
        home_sent(out_home, s)
        home_sent(grad_home, s)

        @pl.when(a != s)
        def _():
            norm_copy(s).wait_send()

        @pl.when(c == 0)
        def _():
            kv_copy(s).wait_send()

        @pl.when(c == 1)
        def _():
            dkv_copy(s).wait_send()

        for index in range(8):
            rows_sent(index, s)
        for p in range(4):

            @pl.when((a == beside(s)) | (a == above(s)))
            def _():
                second_hop(p, s, 0).wait_send()

            @pl.when(a != s)
            def _():
                core_hop(p, s, c).wait_send()

        return 0

    lax.fori_loop(0, lines, sent, 0)


def relay_call(inputs, cotangent, lengths, chosen, singles, weights):
    lines = lax.axis_size("section")
    chips = lax.axis_size("tensor")
    rows, buckets, width = inputs.shape[1:]
    local, total, half = rows * chips, 2 * rows * chips, width // 2
    head_width, units = weights["wo_in"].shape[0], weights["wp_in"].shape[0]
    heads = head_width // HDIM
    stream = local // STREAMS
    peers, owned = chips - 1, stream // 2
    vmem, dma = pltpu.VMEM, pltpu.SemaphoreType.DMA
    operands = dict(
        inputs=inputs,
        cotangent=cotangent,
        lengths=lengths,
        chosen=chosen,
        **singles,
        **weights,
    )

    def space(name):
        if name in weights:
            return pl.ANY
        return pltpu.SMEM if operands[name] is lengths else pltpu.VMEM

    sums = dict(
        acts=((lines, rows, width), LOW),
        grads=((lines, rows, width), LOW),
        ends=((2 * chips, 8, width), F32),
    )
    gathered = dict(
        all_nrm=((lines, 2, STREAMS, stream, half), LOW),
        all_nmlp=((lines, 2, STREAMS, stream, half), LOW),
        all_ups=((lines, 2, STREAMS, stream, half), LOW),
        all_brn=((lines, 2, STREAMS, stream, half), LOW),
        all_act=((lines, 2, STREAMS, stream, units), LOW),
        all_gpre=((lines, 2, STREAMS, stream, units), LOW),
        all_mix=((lines, 2, STREAMS, stream, head_width), LOW),
        all_dqkv=((lines, 2, 3, STREAMS, stream, head_width), LOW),
    )
    outputs = dict(**sums, **gathered)
    scratch = dict(
        wq=vmem((lines,) + weights["wq_in"].shape, LOW),
        wo=vmem((lines,) + weights["wo_in"].shape, LOW),
        wf=vmem((lines,) + weights["wf_in"].shape, LOW),
        wp=vmem((lines,) + weights["wp_in"].shape, LOW),
        small_own=vmem((8, width), F32),
        small=vmem((lines, 8, width), F32),
        count_own=vmem((lines, 8, total), F32),
        count=vmem((lines, 8, total), F32),
        hidden=vmem((STREAMS, owned, width), F32),
        middle=vmem((STREAMS, owned, width), F32),
        upstream=vmem((STREAMS, owned, width), LOW),
        first_out=vmem((2, rows, width), LOW),
        first_in=vmem((2, rows, width), LOW),
        xhat1=vmem((lines, STREAMS, owned, width), F32),
        inv1=vmem((lines, STREAMS, owned, 128), F32),
        xhat2=vmem((lines, STREAMS, owned, width), F32),
        inv2=vmem((lines, STREAMS, owned, 128), F32),
        nrm=vmem((lines, STREAMS, stream, width), LOW),
        nmlp=vmem((lines, STREAMS, stream, width), LOW),
        ups=vmem((lines, STREAMS, stream, width), LOW),
        brn=vmem((lines, STREAMS, stream, width), LOW),
        act=vmem((lines, STREAMS, stream, units), LOW),
        gpre=vmem((lines, STREAMS, stream, units), LOW),
        slope=vmem((lines, STREAMS, stream, units), F32),
        mix=vmem((lines, STREAMS, stream, head_width), LOW),
        qry=vmem((lines, STREAMS, stream, head_width), LOW),
        gmix=vmem((STREAMS, stream, head_width), LOW),
        dqkv=vmem((lines, 3, STREAMS, stream, head_width), LOW),
        kv=vmem((lines, 2, total, head_width), LOW),
        soft=vmem((lines, STREAMS, heads, stream, total), F32),
        near=vmem((STREAMS, stream, total), F32),
        dkv_all=vmem((2, total, head_width), F32),
        dkv_out=vmem((lines, 2, local, head_width), LOW),
        dkv_in=vmem((lines, 2, local, head_width), LOW),
        part=vmem((4, STREAMS, stream, width), LOW),
        arrived=vmem((lines, 4, STREAMS, peers, owned, width), LOW),
        out_low=vmem((lines, 2, rows, width), LOW),
        grad_low=vmem((lines, 2, rows, width), LOW),
        norm_part=vmem((lines, 8, width), F32),
        norm_all=vmem((lines, 8, width), F32),
        w_first_s=dma((4, 2)),
        w_first_r=dma((lines, 4)),
        w_second_s=dma((lines, 4)),
        w_second_r=dma((lines, 4, 2)),
        w_core_s=dma((lines, 4)),
        w_core_r=dma((lines, 4)),
        w_own=dma((4,)),
        small_s=dma((lines - 1,)),
        small_r=dma((lines,)),
        count_s=dma((lines - 1,)),
        count_r=dma((lines,)),
        ag_s=dma((4, STREAMS, peers)),
        ag_r=dma((4, STREAMS, peers)),
        rs_s=dma((4, STREAMS, peers)),
        rs_r=dma((4, STREAMS, peers)),
        kv_s=dma((lines,)),
        kv_r=dma((lines,)),
        dkv_s=dma((lines,)),
        dkv_r=dma((lines,)),
        rows_s=dma((8, lines, 2)),
        rows_r=dma((8,)),
        share_s=dma((4,)),
        share_r=dma((4,)),
        first_s=dma,
        first_r=dma,
        out_s=dma((lines, 2)),
        out_r=dma,
        grad_s=dma((lines, 2)),
        grad_r=dma,
        norm_s=dma((lines,)),
        norm_r=dma,
        ends_s=dma((2 * chips - 1,)),
        ends_r=dma,
    )
    names = tuple(operands) + tuple(outputs) + tuple(scratch)
    results = pl.pallas_call(
        functools.partial(relay_kernel, names),
        out_shape=[jax.ShapeDtypeStruct(shape, kind) for shape, kind in outputs.values()],
        in_specs=[pl.BlockSpec(memory_space=space(name)) for name in operands],
        out_specs=[
            pl.BlockSpec(memory_space=pl.ANY if name in gathered else pltpu.VMEM)
            for name in outputs
        ],
        scratch_shapes=list(scratch.values()),
        compiler_params=pltpu.CompilerParams(
            collective_id=0, has_side_effects=True, vmem_limit_bytes=60 * 2**20
        ),
        name="relay",
    )(*operands.values())
    return dict(zip(outputs, results))


def weights_kernel(names, *refs):
    r = types.SimpleNamespace(**dict(zip(names, refs)))
    step = pl.program_id(0)
    micro_count, rows, buckets, width = r.activations.shape
    chips, units, head_width = r.ends.shape[0] // 2, r.all_act.shape[-1], r.all_mix.shape[-1]

    @pl.when(step == 0)
    def _():
        sums = r.ends[0]
        for other in range(1, 2 * chips):
            sums = sums + r.ends[other]
        singles = (r.ln1_gain, r.ln1_shift, r.ln2_gain, r.ln2_shift, r.b_out, r.b_proj)
        for place, single in enumerate(singles):
            single[...] = sums[place : place + 1]
        for chip in range(chips):
            both = r.ends[chip] + r.ends[chips + chip]
            r.b_fc[:, chip * units : (chip + 1) * units] = both[6:7, :units]
            here = slice(chip * head_width, (chip + 1) * head_width)
            r.b_qv[0:1, here] = both[7:8, :head_width]
            r.b_qv[1:2, here] = both[7:8, width // 2 : width // 2 + head_width]
        for target, source in ((r.activations, r.acts), (r.in_grads, r.grads)):
            for micro in range(micro_count):
                rows_of = [
                    source[micro * buckets + bucket].astype(F32)[:, None, :]
                    for bucket in range(buckets)
                ]
                target[micro] = jnp.concatenate(rows_of, axis=1).astype(LOW)
        for target in (r.w_qkv, r.w_out, r.w_fc, r.w_proj):
            target[...] = jnp.zeros_like(target)

    def rows_of_sequence(ref):
        return ref[0].reshape(2 * chips * rows, ref.shape[-1])

    nrm, nmlp, ups, brn, act, gpre, mix = (
        rows_of_sequence(ref)
        for ref in (r.all_nrm, r.all_nmlp, r.all_ups, r.all_brn, r.all_act, r.all_gpre, r.all_mix)
    )
    r.w_proj[...] += dot_tn(act, ups)
    r.w_fc[...] += dot_tn(nmlp, gpre)
    r.w_out[...] += dot_tn(mix, brn)
    for which in range(3):
        grad = r.all_dqkv[0, :, which].reshape(2 * chips * rows, head_width)
        r.w_qkv[which] += dot_tn(grad, nrm)


def weights_call(relayed, inputs_shape, head_width, units):
    lines = lax.axis_size("section")
    chips = lax.axis_size("tensor")
    width = inputs_shape[-1]
    half = width // 2
    outputs = dict(
        activations=(inputs_shape, LOW),
        in_grads=(inputs_shape, LOW),
        ln1_gain=((1, width), F32),
        ln1_shift=((1, width), F32),
        w_qkv=((3, head_width, half), F32),
        b_qv=((2, width), F32),
        w_out=((head_width, half), F32),
        b_out=((1, width), F32),
        ln2_gain=((1, width), F32),
        ln2_shift=((1, width), F32),
        w_fc=((half, units), F32),
        b_fc=((1, chips * units), F32),
        w_proj=((units, half), F32),
        b_proj=((1, width), F32),
    )

    def spec(array):
        if len(array.shape) < 5:
            return pl.BlockSpec(array.shape, lambda step: (0,) * len(array.shape))
        return pl.BlockSpec(
            (1,) + array.shape[1:], lambda step: (step,) + (0,) * (len(array.shape) - 1)
        )

    def whole(shape):
        return pl.BlockSpec(shape, lambda step: (0,) * len(shape))

    return pl.pallas_call(
        functools.partial(weights_kernel, tuple(relayed) + tuple(outputs)),
        out_shape=[jax.ShapeDtypeStruct(shape, kind) for shape, kind in outputs.values()],
        grid=(lines,),
        in_specs=[spec(array) for array in relayed.values()],
        out_specs=[whole(shape) for shape, _ in outputs.values()],
        compiler_params=pltpu.CompilerParams(vmem_limit_bytes=60 * 2**20),
        name="weight_gradients",
    )(*relayed.values())


def on_line(
    inputs,
    cotangent,
    lengths,
    chosen,
    ln1_gain,
    ln1_shift,
    w_qkv,
    b_qv,
    w_out,
    b_out,
    ln2_gain,
    ln2_shift,
    w_fc,
    b_fc,
    w_proj,
    b_proj,
):
    head_width, units = w_out.shape[1], w_fc.shape[2]
    singles = dict(
        ln1_gain=ln1_gain,
        ln1_shift=ln1_shift,
        ln2_gain=ln2_gain,
        ln2_shift=ln2_shift,
        b_out=b_out,
        b_proj=b_proj,
        b_fc=b_fc,
        b_qv=b_qv[0],
    )
    weights = dict(
        wq_in=jnp.swapaxes(w_qkv[0], 1, 2).reshape(-1, inputs.shape[-1]),
        wo_in=w_out[0],
        wf_in=w_fc[0],
        wp_in=w_proj[0],
    )
    picks = chosen.reshape((-1,) + chosen.shape[-2:])
    relayed = relay_call(inputs, cotangent, lengths, picks, singles, weights)
    results = list(weights_call(relayed, inputs.shape, head_width, units))
    results[4] = jnp.swapaxes(results[4], 1, 2)
    vectors = (2, 3, 7, 8, 9, 11, 13)
    return tuple(
        result if place in vectors else result[None] for place, result in enumerate(results)
    )


def fits_lines(mesh):
    return mesh.shape["section"] == 4 and mesh.shape["seq"] == 2 and mesh.shape["tensor"] == 4


def solution(mesh):
    placed = (
        P(None, ("seq", "tensor"), None, None),
        P(None, ("seq", "tensor"), None, None),
        P(),
        P("section", None, None, "tensor", "seq", None),
        P("section", None),
        P("section", None),
        P("section", None, None, "tensor"),
        P("section", None, "tensor"),
        P("section", "tensor", None),
        P("section", None),
        P("section", None),
        P("section", None),
        P("section", None, "tensor"),
        P("section", "tensor"),
        P("section", "tensor", None),
        P("section", None),
    )
    return jax.shard_map(
        on_line if fits_lines(mesh) else on_device,
        mesh=mesh,
        in_specs=placed,
        out_specs=(
            P("section", None, ("seq", "tensor"), None, None),
            P("section", None, ("seq", "tensor"), None, None),
            P("section", None),
            P("section", None),
            P("section", None, "seq", "tensor"),
            P("section", None, None),
            P("section", "tensor", "seq"),
            P("section", None),
            P("section", None),
            P("section", None),
            P("section", "seq", "tensor"),
            P("section", None),
            P("section", "tensor", "seq"),
            P("section", None),
        ),
        check_vma=False,
    )
```

```python
import functools
import types

import jax
import jax.numpy as jnp
from jax import lax
from jax.experimental import pallas as pl
from jax.experimental.pallas import tpu as pltpu
from jax.sharding import PartitionSpec as P

HDIM = 64
WIN = 64
QB = 64
KSEL = 64


NORM_EPS = 1e-05
MASKED = -1000000000.0


def from_behind(value, axis, steps):
    count = lax.axis_size(axis)
    first, last = (max(0, -steps), min(count, count - steps))
    return lax.ppermute(value, axis, [(source, source + steps) for source in range(first, last)])


def layer_norm(values, gain, shift):
    average = jnp.mean(values, axis=-1, keepdims=True)
    centred = values - average
    variance = jnp.mean(centred * centred, axis=-1, keepdims=True)
    return centred * lax.rsqrt(variance + NORM_EPS) * gain + shift


def gelu_tanh(values):
    return (
        0.5
        * values
        * (1.0 + jnp.tanh(0.7978845608028654 * (values + 0.044715 * values * values * values)))
    )


def gather_rows(row_block):
    return lax.all_gather(row_block, "tensor", axis=0, tiled=True)


def scatter_product(left_rows, weight, formula):
    return lax.psum_scatter(
        jnp.einsum(formula, left_rows, weight, preferred_element_type=jnp.float32).astype(
            jnp.bfloat16
        ),
        "tensor",
        scatter_dimension=0,
        tiled=True,
    ).astype(jnp.float32)


def near_slabs(full_rows, seq_start, seq_first, length_local):
    buckets = full_rows.shape[1]
    heads_local = full_rows.shape[2] // HDIM
    blocks = length_local // QB
    earlier = lax.dynamic_slice_in_dim(full_rows, jnp.maximum(seq_start - WIN, 0), WIN, 0)
    earlier = jnp.where(seq_first, jnp.zeros_like(earlier), earlier)
    local_part = lax.dynamic_slice_in_dim(full_rows, seq_start, length_local, 0)
    segment = jnp.concatenate([earlier, local_part], 0).reshape(
        length_local + WIN, buckets, heads_local, HDIM
    )
    return jnp.concatenate(
        [
            segment[offset_index * QB : offset_index * QB + length_local].reshape(
                blocks, QB, buckets, heads_local, HDIM
            )
            for offset_index in range(WIN // QB + 1)
        ],
        1,
    )


def far_rows(full_rows, flat_index):
    total_rows, buckets, feature_width = full_rows.shape
    heads_local = feature_width // HDIM
    return jnp.take(full_rows.reshape(total_rows * buckets * heads_local, HDIM), flat_index, axis=0)


def key_geometry(chosen_now, seq_start, blocks):
    buckets, heads_local = (chosen_now.shape[0], chosen_now.shape[1])
    bucket_ids = lax.broadcasted_iota(jnp.int32, chosen_now.shape, 0)
    head_ids = lax.broadcasted_iota(jnp.int32, chosen_now.shape, 1)
    flat_index = (chosen_now * buckets + bucket_ids) * heads_local + head_ids
    block_start = seq_start + QB * lax.broadcasted_iota(jnp.int32, (blocks, 1, 1), 0)
    query_ids = lax.broadcasted_iota(jnp.int32, (1, QB, 1), 1)
    key_ids = lax.broadcasted_iota(jnp.int32, (1, 1, WIN + QB), 2)
    distance = query_ids + WIN - key_ids
    near_ok = (distance >= 0) & (distance < WIN) & (block_start + key_ids - WIN >= 0)
    far_ok = chosen_now + WIN <= block_start.reshape(1, 1, blocks, 1)
    near_mask = jnp.broadcast_to(
        near_ok[:, None, None], (blocks, buckets, heads_local, QB, WIN + QB)
    )
    far_mask = jnp.broadcast_to(
        jnp.transpose(far_ok, (2, 0, 1, 3))[:, :, :, None, :],
        (blocks, buckets, heads_local, QB, KSEL),
    )
    return (flat_index, jnp.concatenate([near_mask, far_mask], -1))


def attention_setup(queries, key_rows, value_rows, chosen_now, seq_start, seq_first):
    length_local, buckets, feature_width = queries.shape
    heads_local = feature_width // HDIM
    blocks = length_local // QB
    query_blocks = queries.reshape(blocks, QB, buckets, heads_local, HDIM)
    flat_index, key_mask = key_geometry(chosen_now, seq_start, blocks)
    near_keys = near_slabs(key_rows, seq_start, seq_first, length_local)
    near_values = near_slabs(value_rows, seq_start, seq_first, length_local)
    far_keys = far_rows(key_rows, flat_index)
    far_values = far_rows(value_rows, flat_index)
    near_scores = jnp.einsum(
        "bqnhe,btnhe->bnhqt", query_blocks, near_keys, preferred_element_type=jnp.float32
    )
    far_scores = jnp.einsum(
        "bqnhe,nhbke->bnhqk", query_blocks, far_keys, preferred_element_type=jnp.float32
    )
    scores = jnp.where(
        key_mask, HDIM ** (-0.5) * jnp.concatenate([near_scores, far_scores], -1), MASKED
    )
    return (query_blocks, near_keys, near_values, far_keys, far_values, flat_index, scores)


def attend(queries, key_rows, value_rows, chosen_now, seq_start, seq_first):
    query_blocks, near_keys, near_values, far_keys, far_values, flat_index, scores = (
        attention_setup(queries, key_rows, value_rows, chosen_now, seq_start, seq_first)
    )
    span = WIN + QB
    row_top = jnp.max(scores, -1, keepdims=True)
    exp_terms = jnp.exp(scores - row_top)
    row_total = jnp.sum(exp_terms, -1, keepdims=True)
    softmax_low = (exp_terms / row_total).astype(jnp.bfloat16)
    near_part = jnp.einsum(
        "bnhqt,btnhe->bqnhe",
        softmax_low[..., :span],
        near_values,
        preferred_element_type=jnp.float32,
    )
    far_part = jnp.einsum(
        "bnhqk,nhbke->bqnhe",
        softmax_low[..., span:],
        far_values,
        preferred_element_type=jnp.float32,
    )
    return ((near_part + far_part).reshape(queries.shape), row_top + jnp.log(row_total))


def spread_back(near_grad, far_grad, flat_index, seq_start, seq_first, total_rows):
    blocks, span, buckets, heads_local, head_size = near_grad.shape
    length_local = blocks * QB
    feature_width = heads_local * head_size
    segment = jnp.zeros((length_local + WIN, buckets, heads_local, head_size), jnp.float32)
    for offset_index in range(WIN // QB + 1):
        piece = near_grad[:, offset_index * QB : (offset_index + 1) * QB].reshape(
            length_local, buckets, heads_local, head_size
        )
        segment = segment.at[offset_index * QB : offset_index * QB + length_local].add(piece)
    full_rows = jnp.zeros((total_rows * buckets * heads_local, head_size), jnp.float32)
    full_rows = full_rows.at[flat_index.reshape(-1)].add(far_grad.reshape(-1, head_size))
    full_rows = full_rows.reshape(total_rows, buckets, feature_width)
    local_part = segment[WIN:].reshape(length_local, buckets, feature_width)
    earlier = jnp.where(seq_first, 0.0, segment[:WIN].reshape(WIN, buckets, feature_width))
    full_rows = lax.dynamic_update_slice_in_dim(
        full_rows,
        lax.dynamic_slice_in_dim(full_rows, seq_start, length_local, 0) + local_part,
        seq_start,
        0,
    )
    earlier_start = jnp.maximum(seq_start - WIN, 0)
    full_rows = lax.dynamic_update_slice_in_dim(
        full_rows,
        lax.dynamic_slice_in_dim(full_rows, earlier_start, WIN, 0) + earlier,
        earlier_start,
        0,
    )
    return full_rows


def attend_back(
    queries, key_rows, value_rows, chosen_now, seq_start, seq_first, log_total, grad_mixed
):
    query_blocks, near_keys, near_values, far_keys, far_values, flat_index, scores = (
        attention_setup(queries, key_rows, value_rows, chosen_now, seq_start, seq_first)
    )
    span = WIN + QB
    score_scale = HDIM ** (-0.5)
    grad_blocks = grad_mixed.reshape(query_blocks.shape)
    weights_full = jnp.exp(scores - log_total)
    softmax_low = weights_full.astype(jnp.bfloat16)
    grad_near_weights = jnp.einsum(
        "bqnhe,btnhe->bnhqt", grad_blocks, near_values, preferred_element_type=jnp.float32
    )
    grad_far_weights = jnp.einsum(
        "bqnhe,nhbke->bnhqk", grad_blocks, far_values, preferred_element_type=jnp.float32
    )
    grad_weights = jnp.concatenate([grad_near_weights, grad_far_weights], -1)
    row_dot = jnp.sum(weights_full * grad_weights, -1, keepdims=True)
    grad_scores = (weights_full * (grad_weights - row_dot)).astype(jnp.bfloat16)
    grad_near, grad_far = (grad_scores[..., :span], grad_scores[..., span:])
    grad_queries = score_scale * (
        jnp.einsum("bnhqt,btnhe->bqnhe", grad_near, near_keys, preferred_element_type=jnp.float32)
        + jnp.einsum("bnhqk,nhbke->bqnhe", grad_far, far_keys, preferred_element_type=jnp.float32)
    )
    near_key_grad = score_scale * jnp.einsum(
        "bnhqt,bqnhe->btnhe", grad_near, query_blocks, preferred_element_type=jnp.float32
    )
    far_key_grad = score_scale * jnp.einsum(
        "bnhqk,bqnhe->nhbke", grad_far, query_blocks, preferred_element_type=jnp.float32
    )
    near_value_grad = jnp.einsum(
        "bnhqt,bqnhe->btnhe",
        softmax_low[..., :span],
        grad_blocks,
        preferred_element_type=jnp.float32,
    )
    far_value_grad = jnp.einsum(
        "bnhqk,bqnhe->nhbke",
        softmax_low[..., span:],
        grad_blocks,
        preferred_element_type=jnp.float32,
    )
    total_rows = key_rows.shape[0]
    key_grad = spread_back(
        near_key_grad, far_key_grad, flat_index, seq_start, seq_first, total_rows
    )
    value_grad = spread_back(
        near_value_grad, far_value_grad, flat_index, seq_start, seq_first, total_rows
    )
    return (grad_queries.reshape(queries.shape), key_grad, value_grad)


def forward_pass(hidden, params, chosen_now, query_mask, seq_start, seq_first, finish):
    (
        ln1_gain,
        ln1_shift,
        w_qkv,
        b_qv,
        w_out,
        b_out,
        ln2_gain,
        ln2_shift,
        w_fc,
        b_fc,
        w_proj,
        b_proj,
    ) = params
    hidden_wide = hidden.astype(jnp.float32)
    normed_all = gather_rows(layer_norm(hidden_wide, ln1_gain, ln1_shift).astype(jnp.bfloat16))
    projected = jnp.einsum("pnd,jdc->jpnc", normed_all, w_qkv, preferred_element_type=jnp.float32)
    queries = (projected[0] + b_qv[0]).astype(jnp.bfloat16)
    key_rows, value_rows = (
        lax.all_gather(projected[1].astype(jnp.bfloat16), "seq", axis=0, tiled=True),
        lax.all_gather((projected[2] + b_qv[1]).astype(jnp.bfloat16), "seq", axis=0, tiled=True),
    )
    attended, log_total = attend(queries, key_rows, value_rows, chosen_now, seq_start, seq_first)
    mixed_rows = (attended * query_mask[:, :, None]).astype(jnp.bfloat16)
    middle = hidden_wide + scatter_product(mixed_rows, w_out, "pnc,cd->pnd") + b_out
    normed_mlp = gather_rows(layer_norm(middle, ln2_gain, ln2_shift).astype(jnp.bfloat16))
    pre_active = (
        jnp.einsum("pnd,df->pnf", normed_mlp, w_fc, preferred_element_type=jnp.float32) + b_fc
    )
    active = gelu_tanh(pre_active).astype(jnp.bfloat16)
    if not finish:
        return (
            normed_all,
            queries,
            key_rows,
            value_rows,
            log_total,
            mixed_rows,
            middle,
            normed_mlp,
            pre_active,
            active,
        )
    output = (middle + scatter_product(active, w_proj, "pnf,fd->pnd") + b_proj).astype(jnp.bfloat16)
    return (output, (key_rows, value_rows))


def backward_pass(hidden, upstream, params, chosen_now, query_mask, seq_start, seq_first):
    (
        ln1_gain,
        ln1_shift,
        w_qkv,
        b_qv,
        w_out,
        b_out,
        ln2_gain,
        ln2_shift,
        w_fc,
        b_fc,
        w_proj,
        b_proj,
    ) = params
    (
        normed_all,
        queries,
        key_rows,
        value_rows,
        log_total,
        mixed_rows,
        middle,
        normed_mlp,
        pre_active,
        active,
    ) = forward_pass(hidden, params, chosen_now, query_mask, seq_start, seq_first, False)
    upstream_all = gather_rows(upstream)
    grad_w_proj = jnp.einsum(
        "pnf,pnd->fd", active, upstream_all, preferred_element_type=jnp.float32
    )
    grad_b_proj = jnp.sum(upstream.astype(jnp.float32), axis=(0, 1))
    grad_active = jnp.einsum(
        "pnd,fd->pnf", upstream_all, w_proj, preferred_element_type=jnp.float32
    )
    unused_value, gelu_pull = jax.vjp(gelu_tanh, pre_active)
    grad_pre = gelu_pull(grad_active)[0].astype(jnp.bfloat16)
    grad_w_fc = jnp.einsum("pnd,pnf->df", normed_mlp, grad_pre, preferred_element_type=jnp.float32)
    grad_b_fc = jnp.sum(grad_pre.astype(jnp.float32), axis=(0, 1))
    grad_normed_mlp = scatter_product(grad_pre, w_fc, "pnf,df->pnd")
    unused_norm, second_pull = jax.vjp(layer_norm, middle, ln2_gain, ln2_shift)
    grad_mid_norm, grad_ln2_gain, grad_ln2_shift = second_pull(grad_normed_mlp)
    grad_middle = upstream.astype(jnp.float32) + grad_mid_norm
    grad_branch = grad_middle.astype(jnp.bfloat16)
    grad_b_out = jnp.sum(grad_branch.astype(jnp.float32), axis=(0, 1))
    branch_all = gather_rows(grad_branch)
    grad_w_out = jnp.einsum(
        "pnc,pnd->cd", mixed_rows, branch_all, preferred_element_type=jnp.float32
    )
    grad_mixed = jnp.einsum(
        "pnd,cd->pnc", branch_all, w_out, preferred_element_type=jnp.float32
    ).astype(jnp.bfloat16) * query_mask[:, :, None].astype(jnp.bfloat16)
    grad_queries, key_grad_all, value_grad_all = attend_back(
        queries, key_rows, value_rows, chosen_now, seq_start, seq_first, log_total, grad_mixed
    )
    key_grad, value_grad = (
        lax.psum_scatter(
            key_grad_all.astype(jnp.bfloat16), "seq", scatter_dimension=0, tiled=True
        ).astype(jnp.float32),
        lax.psum_scatter(
            value_grad_all.astype(jnp.bfloat16), "seq", scatter_dimension=0, tiled=True
        ).astype(jnp.float32),
    )
    grad_project = jnp.stack(
        [
            grad_queries.astype(jnp.bfloat16),
            key_grad.astype(jnp.bfloat16),
            value_grad.astype(jnp.bfloat16),
        ],
        2,
    )
    grad_w_qkv = jnp.einsum(
        "pnd,pnjc->jdc", normed_all, grad_project, preferred_element_type=jnp.float32
    )
    grad_b_qv = jnp.sum(grad_project[:, :, 0::2].astype(jnp.float32), axis=(0, 1))
    grad_normed = scatter_product(grad_project, w_qkv, "pnjc,jdc->pnd")
    unused_first, first_pull = jax.vjp(layer_norm, hidden.astype(jnp.float32), ln1_gain, ln1_shift)
    grad_in_norm, grad_ln1_gain, grad_ln1_shift = first_pull(grad_normed)
    grad_hidden = (grad_middle + grad_in_norm).astype(jnp.bfloat16)
    block_grads = (
        grad_ln1_gain,
        grad_ln1_shift,
        grad_w_qkv,
        grad_b_qv,
        grad_w_out,
        grad_b_out,
        grad_ln2_gain,
        grad_ln2_shift,
        grad_w_fc,
        grad_b_fc,
        grad_w_proj,
        grad_b_proj,
    )
    return (grad_hidden, block_grads)


def on_device(
    inputs,
    cotangent,
    lengths,
    chosen,
    ln1_gain,
    ln1_shift,
    w_qkv,
    b_qv,
    w_out,
    b_out,
    ln2_gain,
    ln2_shift,
    w_fc,
    b_fc,
    w_proj,
    b_proj,
):
    params = tuple(
        (
            weight_array[0]
            for weight_array in (
                ln1_gain,
                ln1_shift,
                w_qkv,
                b_qv,
                w_out,
                b_out,
                ln2_gain,
                ln2_shift,
                w_fc,
                b_fc,
                w_proj,
                b_proj,
            )
        )
    )
    section_index = lax.axis_index("section")
    section_count = lax.axis_size("section")
    seq_index = lax.axis_index("seq")
    tensor_index = lax.axis_index("tensor")
    tensor_count = lax.axis_size("tensor")
    micro_count, rows_local, buckets, feature_width = inputs.shape
    length_local = rows_local * tensor_count
    heads_width = w_qkv.shape[-1]
    seq_start = seq_index * length_local
    seq_first = seq_index == 0
    positions = seq_start + lax.broadcasted_iota(jnp.int32, (micro_count, length_local, buckets), 1)
    mask_all = (positions < lengths[:, None, :]).astype(jnp.float32)
    mask_rows = lax.dynamic_slice_in_dim(mask_all, tensor_index * rows_local, rows_local, 1)
    step_count = micro_count + section_count - 1
    chosen_section = chosen[0]
    received = jnp.zeros((rows_local, buckets, feature_width), jnp.bfloat16)
    stored = jnp.zeros((micro_count, rows_local, buckets, feature_width), jnp.bfloat16)
    outputs = jnp.zeros_like(stored)
    for step_index in range(step_count):
        micro_index = step_index - section_index
        running = (micro_index >= 0) & (micro_index < micro_count)
        slot_index = jnp.clip(micro_index, 0, micro_count - 1)
        block_in = jnp.where(
            section_index == 0, lax.dynamic_index_in_dim(inputs, slot_index, 0, False), received
        )
        chosen_now = lax.dynamic_index_in_dim(chosen_section, slot_index, 0, False)
        query_mask = lax.dynamic_index_in_dim(mask_all, slot_index, 0, False)
        result, key_pair = forward_pass(
            block_in, params, chosen_now, query_mask, seq_start, seq_first, True
        )
        stored = jnp.where(
            running, lax.dynamic_update_index_in_dim(stored, block_in, slot_index, 0), stored
        )
        outputs = jnp.where(
            running, lax.dynamic_update_index_in_dim(outputs, result, slot_index, 0), outputs
        )
        received = from_behind(result, "section", 1)
    back_received = jnp.zeros((rows_local, buckets, feature_width), jnp.bfloat16)
    in_grads = jnp.zeros_like(stored)
    totals = None
    for step_index in range(step_count):
        micro_index = step_index - (section_count - 1 - section_index)
        running = (micro_index >= 0) & (micro_index < micro_count)
        slot_index = jnp.clip(micro_index, 0, micro_count - 1)
        chosen_now = lax.dynamic_index_in_dim(chosen_section, slot_index, 0, False)
        query_mask = lax.dynamic_index_in_dim(mask_all, slot_index, 0, False)
        local_mask = lax.dynamic_index_in_dim(mask_rows, slot_index, 0, False)
        top_grad = (
            lax.dynamic_index_in_dim(cotangent, slot_index, 0, False).astype(jnp.float32)
            * local_mask[:, :, None]
        ).astype(jnp.bfloat16)
        upstream = jnp.where(section_index == section_count - 1, top_grad, back_received)
        hidden = lax.dynamic_index_in_dim(stored, slot_index, 0, False)
        grad_hidden, block_grads = backward_pass(
            hidden, upstream, params, chosen_now, query_mask, seq_start, seq_first
        )
        block_grads = tuple(
            (jnp.where(running, grad_part, jnp.zeros_like(grad_part)) for grad_part in block_grads)
        )
        totals = (
            block_grads
            if step_index == 0
            else tuple(
                (total_part + grad_part for total_part, grad_part in zip(totals, block_grads))
            )
        )
        in_grads = jnp.where(
            running, lax.dynamic_update_index_in_dim(in_grads, grad_hidden, slot_index, 0), in_grads
        )
        back_received = from_behind(grad_hidden, "section", -1)
    (
        sum_ln1_gain,
        sum_ln1_shift,
        sum_w_qkv,
        sum_b_qv,
        sum_w_out,
        sum_b_out,
        sum_ln2_gain,
        sum_ln2_shift,
        sum_w_fc,
        sum_b_fc,
        sum_w_proj,
        sum_b_proj,
    ) = totals
    part_qkv, part_out, part_fc, part_proj = (
        lax.psum_scatter(
            sum_w_qkv.astype(jnp.bfloat16), "seq", scatter_dimension=1, tiled=True
        ).astype(jnp.float32),
        lax.psum_scatter(
            sum_w_out.astype(jnp.bfloat16), "seq", scatter_dimension=1, tiled=True
        ).astype(jnp.float32),
        lax.psum_scatter(
            sum_w_fc.astype(jnp.bfloat16), "seq", scatter_dimension=0, tiled=True
        ).astype(jnp.float32),
        lax.psum_scatter(
            sum_w_proj.astype(jnp.bfloat16), "seq", scatter_dimension=1, tiled=True
        ).astype(jnp.float32),
    )
    bias_qv = lax.dynamic_update_slice_in_dim(
        jnp.zeros((2, feature_width), jnp.float32), sum_b_qv, tensor_index * heads_width, 1
    )
    units_local = sum_b_fc.shape[0]
    bias_fc = lax.dynamic_update_slice_in_dim(
        jnp.zeros((units_local * tensor_count,), jnp.float32),
        sum_b_fc,
        tensor_index * units_local,
        0,
    )
    small_sums = lax.psum(
        (
            sum_ln1_gain,
            sum_ln1_shift,
            bias_qv,
            sum_b_out,
            sum_ln2_gain,
            sum_ln2_shift,
            bias_fc,
            sum_b_proj,
        ),
        ("seq", "tensor"),
    )
    return (
        outputs[None],
        in_grads[None],
        small_sums[0][None],
        small_sums[1][None],
        part_qkv[None],
        small_sums[2][None],
        part_out[None],
        small_sums[3][None],
        small_sums[4][None],
        small_sums[5][None],
        part_fc[None],
        small_sums[6][None],
        part_proj[None],
        small_sums[7][None],
    )


STREAMS = 2
NRM, NMLP, UPS, BRN, ACT, GPRE, MIX, DQKV = range(8)
F32 = jnp.float32
LOW = jnp.bfloat16
MESH_ID = pl.DeviceIdType.MESH


def dot_nn(left, right):
    return lax.dot_general(left, right, (((1,), (0,)), ((), ())), preferred_element_type=F32)


def dot_nt(left, right):
    return lax.dot_general(left, right, (((1,), (1,)), ((), ())), preferred_element_type=F32)


def dot_tn(left, right):
    return lax.dot_general(left, right, (((0,), (0,)), ((), ())), preferred_element_type=F32)


def standard(rows):
    centred = rows - jnp.mean(rows, axis=-1, keepdims=True)
    scale = lax.rsqrt(jnp.mean(centred * centred, axis=-1, keepdims=True) + NORM_EPS)
    return centred * scale, scale


def standard_back(grad, xhat, scale):
    inner = jnp.mean(grad * xhat, axis=-1, keepdims=True)
    return scale * (grad - jnp.mean(grad, axis=-1, keepdims=True) - xhat * inner)


def column_sum(rows):
    return jnp.sum(rows.astype(F32), axis=0, keepdims=True)


def relay_kernel(names, *refs):
    r = types.SimpleNamespace(**dict(zip(names, refs)))
    a, c, t = (lax.axis_index(name) for name in ("section", "seq", "tensor"))
    lines = lax.axis_size("section")
    chips = lax.axis_size("tensor")
    rows, buckets, width = r.inputs.shape[1:]
    half_width = width // 2
    local = rows * chips
    total = 2 * local
    stream_rows = local // STREAMS
    head_width = r.wo_in.shape[0]
    heads = head_width // HDIM
    blocks = local // QB
    units = r.wp_in.shape[0]
    scale = HDIM ** (-0.5)
    streams = range(STREAMS)

    def remote(src, dst, send, recv, **target):
        return pltpu.make_async_remote_copy(
            src_ref=src,
            dst_ref=dst,
            send_sem=send,
            recv_sem=recv,
            device_id=target,
            device_id_type=MESH_ID,
        )

    def drain(ref, sem):
        pltpu.make_async_copy(ref, ref, sem).wait()

    def row_block(index, size):
        return pl.ds(pl.multiple_of(index * size, size), size)

    near_chip = t + 1 - 2 * (t % 2)
    over_chip = (t + 2) % 4
    across_chip = 3 - t
    middle_chip = (t == 1) | (t == 2)
    end_chip = (t == 0) | (t == 3)
    owned = stream_rows // 2
    mine = row_block(t - 1, owned)
    my_half = row_block(c, local)

    barrier = pltpu.get_barrier_semaphore()
    for core in range(2):
        for step in range(1, chips):
            there = {"tensor": (t + step) % chips, "seq": core}
            pl.semaphore_signal(barrier, inc=1, device_id=there, device_id_type=MESH_ID)
        for step in range(1, lines):
            there = {"section": (a + step) % lines, "seq": core}
            pl.semaphore_signal(barrier, inc=1, device_id=there, device_id_type=MESH_ID)
    for step in range(1, lines):
        there = {"section": (a + step) % lines, "tensor": near_chip}
        pl.semaphore_signal(barrier, inc=1, device_id=there, device_id_type=MESH_ID)
    pl.semaphore_signal(barrier, inc=1, device_id={"seq": 1 - c}, device_id_type=MESH_ID)
    pl.semaphore_wait(barrier, 2 * (chips - 1) + 3 * (lines - 1) + 1)

    def beside(s):
        return s + 1 - 2 * (s % 2)

    def above(s):
        return (s + 2) % 4

    def store(p):
        return (r.wq, r.wo, r.wf, r.wp)[p]

    def source(p):
        return (r.wq_in, r.wo_in, r.wf_in, r.wp_in)[p]

    def height(p):
        return source(p).shape[0]

    def core_half(p, s, core):
        first = 2 * t if p == 1 else 0
        return store(p).at[s, row_block(first + core, height(p) // 2)]

    def first_hop(p, s, neighbour, which):
        return remote(
            source(p).at[row_block(c, height(p) // 2)],
            core_half(p, s, c),
            r.w_first_s.at[p, which],
            r.w_first_r.at[s, p],
            section=neighbour,
        )

    def second_hop(p, s, which):
        first = 4 * t if p == 1 else 0
        view = store(p).at[s, row_block(first + 2 * c + which, height(p) // 4)]
        return remote(
            view, view, r.w_second_s.at[s, p], r.w_second_r.at[s, p, which], section=3 - s
        )

    def core_hop(p, s, core):
        view = core_half(p, s, core)
        return remote(view, view, r.w_core_s.at[s, p], r.w_core_r.at[s, p], seq=1 - c)

    def own_copy(p):
        place = store(p).at[a, row_block(t, height(p))] if p == 1 else store(p).at[a]
        return pltpu.make_async_copy(source(p), place, r.w_own.at[p])

    def pass_on(s, p, which):
        line = (beside(s), above(s))[which]

        @pl.when(a == line)
        def _():
            first_hop(p, s, line, which).wait_recv()
            second_hop(p, s, which).start()
            core_hop(p, s, c).start()

    def pass_all(s, pieces):
        for p in pieces:
            for which in range(2):
                pass_on(s, p, which)

    def pass_far(s, p):
        @pl.when(a == 3 - s)
        def _():
            second_hop(p, s, 0).wait_recv()
            second_hop(p, s, 1).wait_recv()
            core_hop(p, s, c).start()

    def need(s, p):
        @pl.when(s == 0)
        def _():
            if p < 2:
                pass_all(0, (p,))
            pass_far(0, p)

        @pl.when(a == s)
        def _():
            own_copy(p).wait()

        @pl.when(a != s)
        def _():
            core_hop(p, s, 1 - c).wait_recv()

    def small_copy(step, line, slot):
        return remote(
            r.small_own, r.small.at[slot], r.small_s.at[step], r.small_r.at[slot], section=line
        )

    def count_copy(step, line, slot):
        return remote(
            r.count_own.at[line],
            r.count.at[slot],
            r.count_s.at[step],
            r.count_r.at[slot],
            section=line,
        )

    singles = (r.ln1_gain, r.ln1_shift, r.ln2_gain, r.ln2_shift, r.b_out, r.b_proj)
    for place, single in enumerate(singles):
        r.small_own[place : place + 1] = single[...]
    r.small_own[6:7, :units] = r.b_fc[...]
    r.small_own[7:8, :head_width] = r.b_qv[0:1]
    r.small_own[7:8, half_width : half_width + head_width] = r.b_qv[1:2]
    for step in range(1, lines):
        small_copy(step - 1, (a + step) % lines, a).start()
    for p in range(4):
        for which, line in enumerate((beside(a), above(a))):
            first_hop(p, a, line, which).start()
    for p in range(4):
        own_copy(p).start()
    r.small[a] = r.small_own[...]

    def place_of(index):
        inside = index % local
        stream, left = inside // stream_rows, inside % stream_rows
        first = (index // local) * local + (left // owned) * (local // 2)
        return first + stream * owned + left % owned

    def iota(shape, dimension):
        return lax.broadcasted_iota(jnp.int32, shape, dimension)

    square = jnp.where(iota((KSEL, KSEL), 0) == iota((KSEL, KSEL), 1), 1.0, 0.0).astype(LOW)
    position = place_of(iota((KSEL, total), 1)).astype(F32)
    for pair in range(lines * heads):
        line, head = pair // heads, pair % heads
        columns = dot_nt(square, r.chosen[pair].astype(F32).astype(LOW))
        for block in range(blocks):
            pick = head * blocks + block
            r.count_own[line, pick : pick + 1, :] = jnp.sum(
                jnp.where(columns[:, block : block + 1] == position, 1.0, 0.0),
                axis=0,
                keepdims=True,
            )
    for step in range(1, lines):
        count_copy(step - 1, (a + step) % lines, a).start()
    r.count[a] = r.count_own[a]

    NEAR, OVER, ACROSS = range(3)
    partners = (near_chip, over_chip, across_chip)
    HIDDEN, MIXED, UPSTREAM, CROSS, BRANCH = range(5)

    def spread_copy(s, slot, chip):
        view = r.wo.at[s, row_block(2 * chip + c, head_width // 2)]
        return remote(
            view, view, r.spread_s.at[s, slot], r.spread_r.at[s, slot], tensor=partners[slot]
        )

    def spread_share(s, slot, core):
        view = r.wo.at[s, row_block(2 * partners[slot] + core, head_width // 2)]
        return remote(view, view, r.spread_cs.at[s, slot], r.spread_cr.at[s, slot], seq=1 - c)

    def spread_start(s):
        for slot in range(3):
            spread_copy(s, slot, t).start()

    def spread_pass(s):
        for slot in range(3):
            spread_copy(s, slot, partners[slot]).wait_recv()
            spread_share(s, slot, c).start()

    def spread_ready(s):
        for slot in range(3):
            spread_share(s, slot, 1 - c).wait_recv()

    def mix_copy(s, j, slot, chip):
        view = r.mix.at[s, j, chip]
        return remote(
            view,
            view,
            r.ag_s.at[MIXED, j, slot],
            r.ag_r.at[MIXED, j, slot],
            tensor=partners[slot],
        )

    def cross_copy(s, j, slot):
        return remote(
            r.cross.at[j, partners[slot]],
            r.crossed.at[s, j, slot],
            r.ag_s.at[CROSS, j, slot],
            r.ag_r.at[CROSS, j, slot],
            tensor=partners[slot],
        )

    def exchange_sent(s, kind, j):
        for slot in range(3):
            copy = mix_copy(s, j, slot, t) if kind == MIXED else cross_copy(s, j, slot)
            copy.wait_send()

    def gather(buffer, s, kind, j, owner, target, slot):
        view = buffer.at[s, j, row_block(owner - 1, owned)]
        return remote(
            view, view, r.ag_s.at[kind, j, slot], r.ag_r.at[kind, j, slot], tensor=target
        )

    def used_before(s, kind):
        return s > 0 if kind < UPSTREAM else s < lines - 1

    def gather_start(buffer, s, kind, j):
        @pl.when(used_before(s, kind))
        def _():
            gather_sent(buffer, s, kind, j)

        gather(buffer, s, kind, j, t, over_chip, OVER).start()
        gather(buffer, s, kind, j, t, across_chip, ACROSS).start()
        gather(buffer, s, kind, j, t, near_chip, NEAR).start()

    def gather_wait(buffer, s, kind, j):
        @pl.when(middle_chip)
        def _():
            gather(buffer, s, kind, j, across_chip, across_chip, ACROSS).wait_recv()

        @pl.when(end_chip)
        def _():
            gather(buffer, s, kind, j, near_chip, near_chip, NEAR).wait_recv()
            gather(buffer, s, kind, j, over_chip, over_chip, OVER).wait_recv()

    def gather_sent(buffer, s, kind, j):
        gather(buffer, s, kind, j, t, over_chip, OVER).wait_send()
        gather(buffer, s, kind, j, t, across_chip, ACROSS).wait_send()
        gather(buffer, s, kind, j, t, near_chip, NEAR).wait_send()

    def scatter(s, kind, j, owner, slot):
        return remote(
            r.part.at[kind, j, row_block(owner - 1, owned)],
            r.arrived.at[s, kind, j, slot],
            r.rs_s.at[kind, j, slot],
            r.rs_r.at[kind, j, slot],
            tensor=owner,
        )

    def scatter_start(s, kind, j, product):
        @pl.when(used_before(s, kind))
        def _():
            scatter_sent(s, kind, j)

        r.part[kind, j] = product.astype(LOW)

        @pl.when(end_chip)
        def _():
            scatter(s, kind, j, over_chip, OVER).start()
            scatter(s, kind, j, near_chip, NEAR).start()

        @pl.when(middle_chip)
        def _():
            scatter(s, kind, j, across_chip, ACROSS).start()

    def scatter_sum(s, kind, j):
        result = r.part[kind, j, mine].astype(F32)
        for slot in (NEAR, ACROSS, OVER):
            scatter(s, kind, j, t, slot).wait_recv()
            result = result + r.arrived[s, kind, j, slot].astype(F32)
        return result

    def scatter_sent(s, kind, j):
        @pl.when(end_chip)
        def _():
            scatter(s, kind, j, over_chip, OVER).wait_send()
            scatter(s, kind, j, near_chip, NEAR).wait_send()

        @pl.when(middle_chip)
        def _():
            scatter(s, kind, j, across_chip, ACROSS).wait_send()

    own_rows = (r.nrm, r.nmlp, r.ups, r.brn, r.act, r.gpre, r.mix, r.dqkv)
    all_rows = (
        r.all_nrm,
        r.all_nmlp,
        r.all_ups,
        r.all_brn,
        r.all_act,
        r.all_gpre,
        r.all_mix,
        r.all_dqkv,
    )

    def rows_copy(index, s, same, stays=False):
        core = c if same else 1 - c
        src = r.mix.at[s, :, t] if index == MIX else own_rows[index].at[s]
        dst = all_rows[index].at[a, c]
        if index <= BRN:
            src = src.at[:, :, row_block(core, half_width)]
        recv = r.rows_r.at[index]
        if stays:
            return pltpu.make_async_copy(src, dst, recv)
        if same:
            return remote(src, dst, r.rows_s.at[index, s, 0], recv, section=s)
        return remote(src, dst, r.rows_s.at[index, s, 1], recv, section=s, seq=1 - c)

    def rows_start(index, s):
        @pl.when(a == s)
        def _():
            rows_copy(index, s, True, True).start()

        @pl.when(a != s)
        def _():
            rows_copy(index, s, True).start()

        if index <= BRN:
            rows_copy(index, s, False).start()

    def forward_rows(s):
        for index in (NRM, MIX, NMLP, ACT):
            rows_start(index, s)

    def rows_sent(index, s):
        @pl.when(a != s)
        def _():
            rows_copy(index, s, True).wait_send()

        if index <= BRN:
            rows_copy(index, s, False).wait_send()

    def share_copy(index, core):
        view = all_rows[index].at[:, core]
        return remote(view, view, r.share_s.at[index - ACT], r.share_r.at[index - ACT], seq=1 - c)

    def share(index):
        drain(all_rows[index].at[:, c], r.rows_r.at[index])
        share_copy(index, c).start()

    def norm_copy(s):
        return remote(
            r.norm_part.at[s], r.norm_all.at[a], r.norm_s.at[s], r.norm_r, section=s
        )

    def norm_start(s):
        @pl.when(a == s)
        def _():
            pltpu.make_async_copy(r.norm_part.at[s], r.norm_all.at[a], r.norm_r).start()

        @pl.when(a != s)
        def _():
            norm_copy(s).start()

    def home_copy(what, s, chip):
        src, dst, send, recv = what
        return remote(
            src.at[s, chip % 2],
            dst.at[a],
            send.at[s, chip % 2],
            recv,
            section=s,
            tensor=chip,
        )

    def home_start(what, s):
        src, dst, send, recv = what

        @pl.when(middle_chip & (a == s))
        def _():
            pltpu.make_async_copy(src.at[s, t % 2], dst.at[a], recv).start()

        @pl.when(middle_chip & (a != s))
        def _():
            home_copy(what, s, t).start()

        @pl.when(middle_chip)
        def _():
            home_copy(what, s, near_chip).start()

    def home_sent(what, s):
        @pl.when(middle_chip & (a != s))
        def _():
            home_copy(what, s, t).wait_send()

        @pl.when(middle_chip)
        def _():
            home_copy(what, s, near_chip).wait_send()

    out_home = (r.out_low, r.acts, r.out_s, r.out_r)
    grad_home = (r.grad_low, r.grads, r.grad_s, r.grad_r)

    length = r.lengths[a // buckets, a % buckets]
    key = place_of(iota((stream_rows, total), 1))
    for j in streams:
        query = place_of(c * local + j * stream_rows + iota((stream_rows, total), 0))
        r.near[j] = jnp.where((query >= key) & (query - key < WIN), 1.0, 0.0)
    key_row = place_of(iota((1, total), 1))

    def row_mask(place):
        return jnp.where(place < length, 1.0, 0.0)

    def multiplicity(s, j, head):
        far = []
        for block in range(blocks):
            pick = head * blocks + block
            limit = (c * blocks + block) * QB - WIN
            counted = jnp.where(key_row <= limit, r.count[s, pick : pick + 1, :], 0.0)
            far.append(jnp.broadcast_to(counted, (stream_rows // blocks, total)))
        return r.near[j] + jnp.concatenate(far, axis=0)

    def head_cols(head):
        return slice(head * HDIM, (head + 1) * HDIM)

    def kv_copy(s):
        view = r.kv.at[s, :, 0:local]
        return remote(view, view, r.kv_s.at[s], r.kv_r.at[s], seq=1 - c)

    def dkv_copy(s):
        return remote(r.dkv_out.at[s], r.dkv_in.at[s], r.dkv_s.at[s], r.dkv_r.at[s], seq=1 - c)

    def own_sequence(ref):
        both = ref[a // buckets].astype(F32)
        picked = both[:, 0, :]
        for bucket in range(1, buckets):
            picked = jnp.where(a % buckets == bucket, both[:, bucket, :], picked)
        return picked

    def own_part(j):
        chip, first = (j * owned) // rows, (j * owned) % rows
        return chip, slice(first, first + owned)

    def first_copy():
        return remote(r.first_out, r.first_in, r.first_s, r.first_r, tensor=near_chip)

    own_place = c * local + t * rows + iota((rows, 1), 0)
    r.first_out[0] = own_sequence(r.inputs).astype(LOW)
    r.first_out[1] = (own_sequence(r.cotangent) * row_mask(own_place)).astype(LOW)
    r.norm_part[...] = jnp.zeros_like(r.norm_part)

    @pl.when(c == 0)
    def _():
        r.kv[:, :, local:total] = jnp.zeros((lines, 2, local, head_width), LOW)


    @pl.when(end_chip)
    def _():
        first_copy().start()

    @pl.when(middle_chip)
    def _():
        first_copy().wait_recv()
        for which in range(2):
            here, beside_it = r.first_out[which].astype(F32), r.first_in[which].astype(F32)
            lower = jnp.where(t % 2 == 0, here, beside_it)
            upper = jnp.where(t % 2 == 0, beside_it, here)
            for j in streams:
                chip, part = own_part(j)
                own_block = (lower, upper)[chip][part]
                if which == 0:
                    r.hidden[j] = own_block
                else:
                    r.upstream[j] = own_block.astype(LOW)

    def on_owner(stage):
        def run(s, j):
            @pl.when(middle_chip)
            def _():
                stage(s, j)

        return run

    def keep_rows(target, s, j, result):
        chip, part = own_part(j)
        target[s, chip, part] = result

    @on_owner
    def enter(s, j):
        r.hin[s, j, mine] = r.hidden[j].astype(LOW)
        gather_start(r.hin, s, HIDDEN, j)
        xhat, inverse = standard(r.hidden[j])
        r.xhat1[s, j] = xhat
        r.inv1[s, j] = jnp.broadcast_to(inverse, (owned, 128))

    def project(s, j):
        gather_wait(r.hin, s, HIDDEN, j)
        xhat, _ = standard(r.hin[s, j].astype(F32))
        normed = (xhat * r.small[s, 0:1] + r.small[s, 1:2]).astype(LOW)
        r.nrm[s, j] = normed
        place = row_block(c * STREAMS + j, stream_rows)
        bias_v = r.small[s, 7:8, half_width : half_width + head_width]
        key_rows = dot_nt(normed, r.wq[s, head_width : 2 * head_width])
        value_rows = dot_nt(normed, r.wq[s, 2 * head_width : 3 * head_width]) + bias_v
        r.kv[s, 0, place] = key_rows.astype(LOW)
        r.kv[s, 1, place] = value_rows.astype(LOW)

    def ask(s, j):
        queries = dot_nt(r.nrm[s, j], r.wq[s, 0:head_width]) + r.small[s, 7:8, :head_width]
        r.qry[s, j] = queries.astype(LOW)

    def attend_line(s, j):
        mixed = []
        for head in range(heads):
            cols = head_cols(head)
            times = multiplicity(s, j, head)
            scores = scale * dot_nt(r.qry[s, j, :, cols], r.kv[s, 0, :, cols])
            scores = jnp.where(times > 0.0, scores, MASKED)
            top = jnp.max(scores, axis=-1, keepdims=True)
            terms = times * jnp.exp(scores - top)
            weights = terms / jnp.sum(terms, axis=-1, keepdims=True)
            r.soft[s, j, head] = weights
            mixed.append(dot_nn(weights.astype(LOW), r.kv[s, 1, :, cols]))
        mask = row_mask(place_of(c * local + j * stream_rows + iota((stream_rows, 1), 0)))

        @pl.when(used_before(s, MIXED))
        def _():
            exchange_sent(s, MIXED, j)

        r.mix[s, j, t] = (jnp.concatenate(mixed, axis=-1) * mask).astype(LOW)
        for slot in (OVER, ACROSS, NEAR):
            mix_copy(s, j, slot, t).start()

    def chip_rows(chip):
        return slice(chip * head_width, (chip + 1) * head_width)

    def between(s, j):
        for slot in range(3):
            mix_copy(s, j, slot, partners[slot]).wait_recv()
        middle = r.hin[s, j].astype(F32) + r.small[s, 4:5]
        for chip in range(chips):
            middle = middle + dot_nn(r.mix[s, j, chip], r.wo[s, chip_rows(chip)])
        r.middle[j] = middle
        xhat, inverse = standard(middle)
        r.xhat2[s, j] = xhat
        r.inv2[s, j] = jnp.broadcast_to(inverse, (stream_rows, 128))
        r.nmlp[s, j] = (xhat * r.small[s, 2:3] + r.small[s, 3:4]).astype(LOW)

    def feed(s, j):
        before = dot_nn(r.nmlp[s, j], r.wf[s]) + r.small[s, 6:7, :units]
        bend = jnp.tanh(0.7978845608028654 * (before + 0.044715 * before * before * before))
        r.act[s, j] = (0.5 * before * (1.0 + bend)).astype(LOW)
        r.slope[s, j] = 0.5 * (1.0 + bend) + 0.5 * before * (1.0 - bend * bend) * (
            0.7978845608028654 * (1.0 + 3 * 0.044715 * before * before)
        )


    def leave_feed(s, j):
        scatter_start(s, 1, j, dot_nn(r.act[s, j], r.wp[s]))

    @on_owner
    def finish(s, j):
        result = r.middle[j, mine] + scatter_sum(s, 1, j) + r.small[s, 5:6]
        keep_rows(r.out_low, s, j, result.astype(LOW))
        r.hidden[j] = result.astype(LOW).astype(F32)

    def small_ready(s):
        @pl.when(a != s)
        def _():
            small_copy(0, a, s).wait_recv()

    small_ready(0)
    for j in streams:
        enter(0, j)

    def forward(s, _):
        need(s, 0)

        @pl.when(s == 0)
        def _():
            need(0, 1)
            spread_start(0)

        for j in streams:
            project(s, j)

        @pl.when(c == 0)
        def _():
            kv_copy(s).start()

        for j in streams:
            ask(s, j)

        @pl.when(a != s)
        def _():
            count_copy(0, a, s).wait_recv()

        @pl.when(c == 1)
        def _():
            kv_copy(s).wait_recv()

        for j in streams:
            attend_line(s, j)
            if j == 0:
                spread_pass(s)


        @pl.when(s == 0)
        def _():
            pass_all(0, (2,))
            for later in range(1, lines):
                pass_all(later, (0, 1, 2))

        @pl.when(s == 1)
        def _():
            pass_far(1, 2)
            pass_far(1, 3)
            for later in range(2, lines):
                for p in range(4):
                    pass_far(later, p)

        @pl.when(s == 0)
        def _():
            for later in range(lines):
                pass_all(later, (3,))

        spread_ready(s)
        need(s, 2)
        for j in streams:
            between(s, j)
            feed(s, j)
            if j == 0:
                need(s, 3)
            leave_feed(s, j)


        @pl.when(s >= 2)
        def _():
            forward_rows(s - 2)


        @pl.when(s + 1 < lines)
        def _():
            small_ready(s + 1)

        for j in streams:
            finish(s, j)

            @pl.when(s + 1 < lines)
            def _():
                enter(s + 1, j)

        home_start(out_home, s)

        @pl.when(s == 0)
        def _():
            pass_far(1, 0)
            pass_far(1, 1)

        @pl.when(s + 1 < lines)
        def _():
            need(s + 1, 1)
            spread_start(s + 1)

        return 0

    lax.fori_loop(0, lines, forward, 0)

    @on_owner
    def turn(s, j):
        upstream = r.upstream[j]
        r.ups[s, j, mine] = upstream
        gather_start(r.ups, s, UPSTREAM, j)
        r.norm_part[s, 5:6] += column_sum(upstream)

    def split_low(values):
        high = values.astype(LOW).astype(F32)
        return high, values - high

    def feed_back(s, j):
        gather_wait(r.ups, s, UPSTREAM, j)
        grad_pre = (dot_nt(r.ups[s, j], r.wp[s]) * r.slope[s, j]).astype(LOW)
        r.gpre[s, j] = grad_pre
        grad = dot_nt(grad_pre, r.wf[s])
        scaled = grad * r.small[s, 2:3]
        scaled_low = scaled.astype(LOW)
        means = split_low(jnp.mean(scaled, axis=-1, keepdims=True))
        means += split_low(jnp.mean(scaled * r.xhat2[s, j], axis=-1, keepdims=True))
        lane = iota((stream_rows, HDIM), 1)
        packed = jnp.zeros((stream_rows, HDIM), F32)
        for place, mean in enumerate(means):
            packed = jnp.where(lane == place, mean, packed)

        @pl.when(used_before(s, CROSS))
        def _():
            exchange_sent(s, CROSS, j)

        for chip in range(chips):
            share = dot_nt(scaled_low, r.wo[s, chip_rows(chip)])
            r.cross[j, chip, :, 0:head_width] = share.astype(LOW)
            r.cross[j, chip, :, head_width : head_width + HDIM] = packed.astype(LOW)
        for slot in (OVER, ACROSS, NEAR):
            cross_copy(s, j, slot).start()
        scatter_start(s, 2, j, grad)
        r.norm_part[s, 6:7, :units] += column_sum(grad_pre)

    @on_owner
    def between_back(s, j):
        grad = scatter_sum(s, 2, j)
        xhat = r.xhat2[s, j, mine]
        upstream = r.upstream[j].astype(F32)
        grad_middle = upstream + standard_back(
            grad * r.small[s, 2:3], xhat, r.inv2[s, j, mine, 0:1]
        )
        r.gmid[j] = grad_middle
        branch = grad_middle.astype(LOW)
        r.brn[s, j, mine] = branch
        gather_start(r.brn, s, BRANCH, j)
        r.norm_part[s, 2:3] += column_sum(grad * xhat)
        r.norm_part[s, 3:4] += column_sum(grad)
        r.norm_part[s, 4:5] += column_sum(branch)

    def mixed_back(s, j):
        own = row_block(t, head_width)
        through = dot_nt(r.ups[s, j], r.wo[s, own])
        along = dot_nt(r.xhat2[s, j].astype(LOW), r.wo[s, own])
        ones = dot_nt(jnp.ones((16, width), LOW), r.wo[s, own])[0:1]
        total_share = r.cross[j, t].astype(F32)
        for slot in range(3):
            cross_copy(s, j, slot).wait_recv()
            total_share = total_share + r.crossed[s, j, slot].astype(F32)
        first = head_width
        mean = total_share[:, first : first + 1] + total_share[:, first + 1 : first + 2]
        lean = total_share[:, first + 2 : first + 3] + total_share[:, first + 3 : first + 4]
        inner = total_share[:, 0:head_width] - mean * ones - lean * along
        place = place_of(c * local + j * stream_rows + iota((stream_rows, 1), 0))
        grad_mixed = through + r.inv2[s, j, :, 0:1] * inner
        r.gmix[j] = (grad_mixed * row_mask(place)).astype(LOW)

    def branch_ready(s):
        for j in streams:
            gather_wait(r.brn, s, BRANCH, j)

    def attend_line_back(s, j):
        grad_q, grad_k, grad_v = [], [], []
        for head in range(heads):
            cols = head_cols(head)
            weights = r.soft[s, j, head]
            grad_head = r.gmix[j, :, cols]
            grad_weights = dot_nt(grad_head, r.kv[s, 1, :, cols])
            inner = jnp.sum(weights * grad_weights, axis=-1, keepdims=True)
            grad_scores = (weights * (grad_weights - inner)).astype(LOW)
            grad_k.append(scale * dot_tn(grad_scores, r.qry[s, j, :, cols]))
            grad_v.append(dot_tn(weights.astype(LOW), grad_head))
            grad_q.append(scale * dot_nn(grad_scores, r.kv[s, 0, :, cols]))
        for which, grad in enumerate((grad_k, grad_v)):
            grad = jnp.concatenate(grad, axis=-1)
            r.dkv_all[which] = grad if j == 0 else r.dkv_all[which] + grad
        grad_q = jnp.concatenate(grad_q, axis=-1).astype(LOW)
        r.dqkv[s, 0, j] = grad_q
        r.norm_part[s, 7:8, :head_width] += column_sum(grad_q)

    def join_keys(s):
        @pl.when(c == 1)
        def _():
            r.dkv_out[s] = r.dkv_all[:, 0:local].astype(LOW)
            dkv_copy(s).start()

        @pl.when(c == 0)
        def _():
            dkv_copy(s).wait_recv()
            r.dkv_all[:, 0:local] += r.dkv_in[s].astype(F32)

        for which in range(2):
            joined = r.dkv_all[which, my_half].astype(LOW)
            r.dqkv[s, 1 + which] = joined.reshape(r.dqkv.shape[2:])
            if which == 1:
                r.norm_part[s, 7:8, half_width : half_width + head_width] = column_sum(joined)

    def leave_back(s, j):
        product = dot_nn(r.dqkv[s, 0, j], r.wq[s, 0:head_width])
        for which in range(1, 3):
            weight = r.wq[s, which * head_width : (which + 1) * head_width]
            product = product + dot_nn(r.dqkv[s, which, j], weight)
        scatter_start(s, 3, j, product)

    @on_owner
    def finish_back(s, j):
        grad = scatter_sum(s, 3, j)
        xhat = r.xhat1[s, j]
        result = r.gmid[j] + standard_back(
            grad * r.small[s, 0:1], xhat, r.inv1[s, j, :, 0:1]
        )
        r.upstream[j] = result.astype(LOW)
        keep_rows(r.grad_low, s, j, result.astype(LOW))
        r.norm_part[s, 0:1] += column_sum(grad * xhat)
        r.norm_part[s, 1:2] += column_sum(grad)

    for j in streams:
        turn(lines - 1, j)

    def backward(index, _):
        s = lines - 1 - index

        @pl.when(index > 0)
        def _():
            branch_ready(s + 1)

        for j in streams:
            feed_back(s, j)
        rows_start(UPS, s)
        rows_start(GPRE, s)

        @pl.when(index > 0)
        def _():
            rows_start(BRN, s + 1)

        @pl.when(index < 2)
        def _():
            forward_rows(lines - 2 + index)

        @pl.when(index == lines - 1)
        def _():
            share(ACT)
            share(MIX)

        for j in streams:
            mixed_back(s, j)
            attend_line_back(s, j)
        join_keys(s)
        for j in streams:
            leave_back(s, j)
        rows_start(DQKV, s)
        for j in streams:
            between_back(s, j)
        for j in streams:
            finish_back(s, j)

            @pl.when(s > 0)
            def _():
                turn(s - 1, j)

        norm_start(s)
        home_start(grad_home, s)
        return 0

    lax.fori_loop(0, lines, backward, 0)

    branch_ready(0)
    rows_start(BRN, 0)
    share(GPRE)
    share(DQKV)

    drain(r.norm_all, r.norm_r)
    slot = c * chips + t
    norm_sum = r.norm_all[0]
    for line in range(1, lines):
        norm_sum = norm_sum + r.norm_all[line]
    r.ends[slot] = norm_sum

    def ends_copy(step):
        core, chip = step // chips, step % chips
        view = r.ends.at[slot]
        return remote(
            view,
            view,
            r.ends_s.at[step - 1],
            r.ends_r,
            seq=(c + core) % 2,
            tensor=(t + chip) % chips,
        )

    for step in range(1, 2 * chips):
        ends_copy(step).start()

    for j in streams:
        exchange_sent(0, MIXED, j)
        exchange_sent(0, CROSS, j)
        for kind in range(1, 4):
            scatter_sent(0, kind, j)

        @pl.when(middle_chip)
        def _():
            for kind, buffer in ((HIDDEN, r.hin), (UPSTREAM, r.ups), (BRANCH, r.brn)):
                gather_sent(buffer, 0, kind, j)

    for index in range(ACT):
        drain(all_rows[index], r.rows_r.at[index])
    for index in range(ACT, 8):
        share_copy(index, 1 - c).wait_recv()
        share_copy(index, c).wait_send()
    drain(r.acts, r.out_r)
    drain(r.grads, r.grad_r)
    drain(r.ends.at[0 : 2 * chips - 1], r.ends_r)
    for step in range(1, 2 * chips):
        ends_copy(step).wait_send()
    for step in range(1, lines):
        small_copy(step - 1, (a + step) % lines, a).wait_send()
        count_copy(step - 1, (a + step) % lines, a).wait_send()
    for p in range(4):
        for which, line in enumerate((beside(a), above(a))):
            first_hop(p, a, line, which).wait_send()

    @pl.when(end_chip)
    def _():
        first_copy().wait_send()

    def sent(s, _):
        for slot in range(3):
            spread_copy(s, slot, t).wait_send()
            spread_share(s, slot, c).wait_send()

        home_sent(out_home, s)
        home_sent(grad_home, s)

        @pl.when(a != s)
        def _():
            norm_copy(s).wait_send()

        @pl.when(c == 0)
        def _():
            kv_copy(s).wait_send()

        @pl.when(c == 1)
        def _():
            dkv_copy(s).wait_send()

        for index in range(8):
            rows_sent(index, s)
        for p in range(4):

            @pl.when((a == beside(s)) | (a == above(s)))
            def _():
                second_hop(p, s, 0).wait_send()

            @pl.when(a != s)
            def _():
                core_hop(p, s, c).wait_send()

        return 0

    lax.fori_loop(0, lines, sent, 0)


def relay_call(inputs, cotangent, lengths, chosen, singles, weights):
    lines = lax.axis_size("section")
    chips = lax.axis_size("tensor")
    rows, buckets, width = inputs.shape[1:]
    local, total, half = rows * chips, 2 * rows * chips, width // 2
    head_width, units = weights["wo_in"].shape[0], weights["wp_in"].shape[0]
    heads = head_width // HDIM
    stream = local // STREAMS
    peers, owned = chips - 1, stream // 2
    vmem, dma = pltpu.VMEM, pltpu.SemaphoreType.DMA
    operands = dict(
        inputs=inputs,
        cotangent=cotangent,
        lengths=lengths,
        chosen=chosen,
        **singles,
        **weights,
    )

    def space(name):
        if name in weights:
            return pl.ANY
        return pltpu.SMEM if operands[name] is lengths else pltpu.VMEM

    sums = dict(
        acts=((lines, rows, width), LOW),
        grads=((lines, rows, width), LOW),
        ends=((2 * chips, 8, width), F32),
    )
    gathered = dict(
        all_nrm=((lines, 2, STREAMS, stream, half), LOW),
        all_nmlp=((lines, 2, STREAMS, stream, half), LOW),
        all_ups=((lines, 2, STREAMS, stream, half), LOW),
        all_brn=((lines, 2, STREAMS, stream, half), LOW),
        all_act=((lines, 2, STREAMS, stream, units), LOW),
        all_gpre=((lines, 2, STREAMS, stream, units), LOW),
        all_mix=((lines, 2, STREAMS, stream, head_width), LOW),
        all_dqkv=((lines, 2, 3, STREAMS, stream, head_width), LOW),
    )
    outputs = dict(**sums, **gathered)
    scratch = dict(
        wq=vmem((lines,) + weights["wq_in"].shape, LOW),
        wo=vmem((lines, chips * head_width, width), LOW),
        wf=vmem((lines,) + weights["wf_in"].shape, LOW),
        wp=vmem((lines,) + weights["wp_in"].shape, LOW),
        small_own=vmem((8, width), F32),
        small=vmem((lines, 8, width), F32),
        count_own=vmem((lines, 8, total), F32),
        count=vmem((lines, 8, total), F32),
        hidden=vmem((STREAMS, owned, width), F32),
        middle=vmem((STREAMS, stream, width), F32),
        gmid=vmem((STREAMS, owned, width), F32),
        hin=vmem((lines, STREAMS, stream, width), LOW),
        cross=vmem((STREAMS, chips, stream, head_width + HDIM), LOW),
        crossed=vmem((lines, STREAMS, peers, stream, head_width + HDIM), LOW),
        upstream=vmem((STREAMS, owned, width), LOW),
        first_out=vmem((2, rows, width), LOW),
        first_in=vmem((2, rows, width), LOW),
        xhat1=vmem((lines, STREAMS, owned, width), F32),
        inv1=vmem((lines, STREAMS, owned, 128), F32),
        xhat2=vmem((lines, STREAMS, stream, width), F32),
        inv2=vmem((lines, STREAMS, stream, 128), F32),
        nrm=vmem((lines, STREAMS, stream, width), LOW),
        nmlp=vmem((lines, STREAMS, stream, width), LOW),
        ups=vmem((lines, STREAMS, stream, width), LOW),
        brn=vmem((lines, STREAMS, stream, width), LOW),
        act=vmem((lines, STREAMS, stream, units), LOW),
        gpre=vmem((lines, STREAMS, stream, units), LOW),
        slope=vmem((lines, STREAMS, stream, units), F32),
        mix=vmem((lines, STREAMS, chips, stream, head_width), LOW),
        qry=vmem((lines, STREAMS, stream, head_width), LOW),
        gmix=vmem((STREAMS, stream, head_width), LOW),
        dqkv=vmem((lines, 3, STREAMS, stream, head_width), LOW),
        kv=vmem((lines, 2, total, head_width), LOW),
        soft=vmem((lines, STREAMS, heads, stream, total), F32),
        near=vmem((STREAMS, stream, total), F32),
        dkv_all=vmem((2, total, head_width), F32),
        dkv_out=vmem((lines, 2, local, head_width), LOW),
        dkv_in=vmem((lines, 2, local, head_width), LOW),
        part=vmem((4, STREAMS, stream, width), LOW),
        arrived=vmem((lines, 4, STREAMS, peers, owned, width), LOW),
        out_low=vmem((lines, 2, rows, width), LOW),
        grad_low=vmem((lines, 2, rows, width), LOW),
        norm_part=vmem((lines, 8, width), F32),
        norm_all=vmem((lines, 8, width), F32),
        w_first_s=dma((4, 2)),
        w_first_r=dma((lines, 4)),
        w_second_s=dma((lines, 4)),
        w_second_r=dma((lines, 4, 2)),
        w_core_s=dma((lines, 4)),
        w_core_r=dma((lines, 4)),
        w_own=dma((4,)),
        spread_s=dma((lines, peers)),
        spread_r=dma((lines, peers)),
        spread_cs=dma((lines, peers)),
        spread_cr=dma((lines, peers)),
        small_s=dma((lines - 1,)),
        small_r=dma((lines,)),
        count_s=dma((lines - 1,)),
        count_r=dma((lines,)),
        ag_s=dma((5, STREAMS, peers)),
        ag_r=dma((5, STREAMS, peers)),
        rs_s=dma((4, STREAMS, peers)),
        rs_r=dma((4, STREAMS, peers)),
        kv_s=dma((lines,)),
        kv_r=dma((lines,)),
        dkv_s=dma((lines,)),
        dkv_r=dma((lines,)),
        rows_s=dma((8, lines, 2)),
        rows_r=dma((8,)),
        share_s=dma((4,)),
        share_r=dma((4,)),
        first_s=dma,
        first_r=dma,
        out_s=dma((lines, 2)),
        out_r=dma,
        grad_s=dma((lines, 2)),
        grad_r=dma,
        norm_s=dma((lines,)),
        norm_r=dma,
        ends_s=dma((2 * chips - 1,)),
        ends_r=dma,
    )
    names = tuple(operands) + tuple(outputs) + tuple(scratch)
    results = pl.pallas_call(
        functools.partial(relay_kernel, names),
        out_shape=[jax.ShapeDtypeStruct(shape, kind) for shape, kind in outputs.values()],
        in_specs=[pl.BlockSpec(memory_space=space(name)) for name in operands],
        out_specs=[
            pl.BlockSpec(memory_space=pl.ANY if name in gathered else pltpu.VMEM)
            for name in outputs
        ],
        scratch_shapes=list(scratch.values()),
        compiler_params=pltpu.CompilerParams(
            collective_id=0, has_side_effects=True, vmem_limit_bytes=60 * 2**20
        ),
        name="relay",
    )(*operands.values())
    return dict(zip(outputs, results))


def weights_kernel(names, *refs):
    r = types.SimpleNamespace(**dict(zip(names, refs)))
    step = pl.program_id(0)
    micro_count, rows, buckets, width = r.activations.shape
    chips, units, head_width = r.ends.shape[0] // 2, r.all_act.shape[-1], r.all_mix.shape[-1]

    @pl.when(step == 0)
    def _():
        sums = r.ends[0]
        for other in range(1, 2 * chips):
            sums = sums + r.ends[other]
        singles = (r.ln1_gain, r.ln1_shift, r.ln2_gain, r.ln2_shift, r.b_out, r.b_proj)
        for place, single in enumerate(singles):
            single[...] = sums[place : place + 1]
        for chip in range(chips):
            both = r.ends[chip] + r.ends[chips + chip]
            r.b_fc[:, chip * units : (chip + 1) * units] = both[6:7, :units]
            here = slice(chip * head_width, (chip + 1) * head_width)
            r.b_qv[0:1, here] = both[7:8, :head_width]
            r.b_qv[1:2, here] = both[7:8, width // 2 : width // 2 + head_width]
        for target, source in ((r.activations, r.acts), (r.in_grads, r.grads)):
            for micro in range(micro_count):
                rows_of = [
                    source[micro * buckets + bucket].astype(F32)[:, None, :]
                    for bucket in range(buckets)
                ]
                target[micro] = jnp.concatenate(rows_of, axis=1).astype(LOW)
        for target in (r.w_qkv, r.w_out, r.w_fc, r.w_proj):
            target[...] = jnp.zeros_like(target)

    def rows_of_sequence(ref):
        return ref[0].reshape(2 * chips * rows, ref.shape[-1])

    nrm, nmlp, ups, brn, act, gpre, mix = (
        rows_of_sequence(ref)
        for ref in (r.all_nrm, r.all_nmlp, r.all_ups, r.all_brn, r.all_act, r.all_gpre, r.all_mix)
    )
    r.w_proj[...] += dot_tn(act, ups)
    r.w_fc[...] += dot_tn(nmlp, gpre)
    r.w_out[...] += dot_tn(mix, brn)
    for which in range(3):
        grad = r.all_dqkv[0, :, which].reshape(2 * chips * rows, head_width)
        r.w_qkv[which] += dot_tn(grad, nrm)


def weights_call(relayed, inputs_shape, head_width, units):
    lines = lax.axis_size("section")
    chips = lax.axis_size("tensor")
    width = inputs_shape[-1]
    half = width // 2
    outputs = dict(
        activations=(inputs_shape, LOW),
        in_grads=(inputs_shape, LOW),
        ln1_gain=((1, width), F32),
        ln1_shift=((1, width), F32),
        w_qkv=((3, head_width, half), F32),
        b_qv=((2, width), F32),
        w_out=((head_width, half), F32),
        b_out=((1, width), F32),
        ln2_gain=((1, width), F32),
        ln2_shift=((1, width), F32),
        w_fc=((half, units), F32),
        b_fc=((1, chips * units), F32),
        w_proj=((units, half), F32),
        b_proj=((1, width), F32),
    )

    def spec(array):
        if len(array.shape) < 5:
            return pl.BlockSpec(array.shape, lambda step: (0,) * len(array.shape))
        return pl.BlockSpec(
            (1,) + array.shape[1:], lambda step: (step,) + (0,) * (len(array.shape) - 1)
        )

    def whole(shape):
        return pl.BlockSpec(shape, lambda step: (0,) * len(shape))

    return pl.pallas_call(
        functools.partial(weights_kernel, tuple(relayed) + tuple(outputs)),
        out_shape=[jax.ShapeDtypeStruct(shape, kind) for shape, kind in outputs.values()],
        grid=(lines,),
        in_specs=[spec(array) for array in relayed.values()],
        out_specs=[whole(shape) for shape, _ in outputs.values()],
        compiler_params=pltpu.CompilerParams(vmem_limit_bytes=60 * 2**20),
        name="weight_gradients",
    )(*relayed.values())


def on_line(
    inputs,
    cotangent,
    lengths,
    chosen,
    ln1_gain,
    ln1_shift,
    w_qkv,
    b_qv,
    w_out,
    b_out,
    ln2_gain,
    ln2_shift,
    w_fc,
    b_fc,
    w_proj,
    b_proj,
):
    head_width, units = w_out.shape[1], w_fc.shape[2]
    singles = dict(
        ln1_gain=ln1_gain,
        ln1_shift=ln1_shift,
        ln2_gain=ln2_gain,
        ln2_shift=ln2_shift,
        b_out=b_out,
        b_proj=b_proj,
        b_fc=b_fc,
        b_qv=b_qv[0],
    )
    weights = dict(
        wq_in=jnp.swapaxes(w_qkv[0], 1, 2).reshape(-1, inputs.shape[-1]),
        wo_in=w_out[0],
        wf_in=w_fc[0],
        wp_in=w_proj[0],
    )
    picks = chosen.reshape((-1,) + chosen.shape[-2:])
    relayed = relay_call(inputs, cotangent, lengths, picks, singles, weights)
    results = list(weights_call(relayed, inputs.shape, head_width, units))
    results[4] = jnp.swapaxes(results[4], 1, 2)
    vectors = (2, 3, 7, 8, 9, 11, 13)
    return tuple(
        result if place in vectors else result[None] for place, result in enumerate(results)
    )


def fits_lines(mesh):
    return mesh.shape["section"] == 4 and mesh.shape["seq"] == 2 and mesh.shape["tensor"] == 4


def solution(mesh):
    placed = (
        P(None, ("seq", "tensor"), None, None),
        P(None, ("seq", "tensor"), None, None),
        P(),
        P("section", None, None, "tensor", "seq", None),
        P("section", None),
        P("section", None),
        P("section", None, None, "tensor"),
        P("section", None, "tensor"),
        P("section", "tensor", None),
        P("section", None),
        P("section", None),
        P("section", None),
        P("section", None, "tensor"),
        P("section", "tensor"),
        P("section", "tensor", None),
        P("section", None),
    )
    return jax.shard_map(
        on_line if fits_lines(mesh) else on_device,
        mesh=mesh,
        in_specs=placed,
        out_specs=(
            P("section", None, ("seq", "tensor"), None, None),
            P("section", None, ("seq", "tensor"), None, None),
            P("section", None),
            P("section", None),
            P("section", None, "seq", "tensor"),
            P("section", None, None),
            P("section", "tensor", "seq"),
            P("section", None),
            P("section", None),
            P("section", None),
            P("section", "seq", "tensor"),
            P("section", None),
            P("section", "tensor", "seq"),
            P("section", None),
        ),
        check_vma=False,
    )
```

```python
import functools
import types

import jax
import jax.numpy as jnp
from jax import lax
from jax.experimental import pallas as pl
from jax.experimental.pallas import tpu as pltpu
from jax.sharding import PartitionSpec as P

HDIM = 64
WIN = 64
QB = 64
KSEL = 64


NORM_EPS = 1e-05
MASKED = -1000000000.0


def from_behind(value, axis, steps):
    count = lax.axis_size(axis)
    first, last = (max(0, -steps), min(count, count - steps))
    return lax.ppermute(value, axis, [(source, source + steps) for source in range(first, last)])


def layer_norm(values, gain, shift):
    average = jnp.mean(values, axis=-1, keepdims=True)
    centred = values - average
    variance = jnp.mean(centred * centred, axis=-1, keepdims=True)
    return centred * lax.rsqrt(variance + NORM_EPS) * gain + shift


def gelu_tanh(values):
    return (
        0.5
        * values
        * (1.0 + jnp.tanh(0.7978845608028654 * (values + 0.044715 * values * values * values)))
    )


def gather_rows(row_block):
    return lax.all_gather(row_block, "tensor", axis=0, tiled=True)


def scatter_product(left_rows, weight, formula):
    return lax.psum_scatter(
        jnp.einsum(formula, left_rows, weight, preferred_element_type=jnp.float32).astype(
            jnp.bfloat16
        ),
        "tensor",
        scatter_dimension=0,
        tiled=True,
    ).astype(jnp.float32)


def near_slabs(full_rows, seq_start, seq_first, length_local):
    buckets = full_rows.shape[1]
    heads_local = full_rows.shape[2] // HDIM
    blocks = length_local // QB
    earlier = lax.dynamic_slice_in_dim(full_rows, jnp.maximum(seq_start - WIN, 0), WIN, 0)
    earlier = jnp.where(seq_first, jnp.zeros_like(earlier), earlier)
    local_part = lax.dynamic_slice_in_dim(full_rows, seq_start, length_local, 0)
    segment = jnp.concatenate([earlier, local_part], 0).reshape(
        length_local + WIN, buckets, heads_local, HDIM
    )
    return jnp.concatenate(
        [
            segment[offset_index * QB : offset_index * QB + length_local].reshape(
                blocks, QB, buckets, heads_local, HDIM
            )
            for offset_index in range(WIN // QB + 1)
        ],
        1,
    )


def far_rows(full_rows, flat_index):
    total_rows, buckets, feature_width = full_rows.shape
    heads_local = feature_width // HDIM
    return jnp.take(full_rows.reshape(total_rows * buckets * heads_local, HDIM), flat_index, axis=0)


def key_geometry(chosen_now, seq_start, blocks):
    buckets, heads_local = (chosen_now.shape[0], chosen_now.shape[1])
    bucket_ids = lax.broadcasted_iota(jnp.int32, chosen_now.shape, 0)
    head_ids = lax.broadcasted_iota(jnp.int32, chosen_now.shape, 1)
    flat_index = (chosen_now * buckets + bucket_ids) * heads_local + head_ids
    block_start = seq_start + QB * lax.broadcasted_iota(jnp.int32, (blocks, 1, 1), 0)
    query_ids = lax.broadcasted_iota(jnp.int32, (1, QB, 1), 1)
    key_ids = lax.broadcasted_iota(jnp.int32, (1, 1, WIN + QB), 2)
    distance = query_ids + WIN - key_ids
    near_ok = (distance >= 0) & (distance < WIN) & (block_start + key_ids - WIN >= 0)
    far_ok = chosen_now + WIN <= block_start.reshape(1, 1, blocks, 1)
    near_mask = jnp.broadcast_to(
        near_ok[:, None, None], (blocks, buckets, heads_local, QB, WIN + QB)
    )
    far_mask = jnp.broadcast_to(
        jnp.transpose(far_ok, (2, 0, 1, 3))[:, :, :, None, :],
        (blocks, buckets, heads_local, QB, KSEL),
    )
    return (flat_index, jnp.concatenate([near_mask, far_mask], -1))


def attention_setup(queries, key_rows, value_rows, chosen_now, seq_start, seq_first):
    length_local, buckets, feature_width = queries.shape
    heads_local = feature_width // HDIM
    blocks = length_local // QB
    query_blocks = queries.reshape(blocks, QB, buckets, heads_local, HDIM)
    flat_index, key_mask = key_geometry(chosen_now, seq_start, blocks)
    near_keys = near_slabs(key_rows, seq_start, seq_first, length_local)
    near_values = near_slabs(value_rows, seq_start, seq_first, length_local)
    far_keys = far_rows(key_rows, flat_index)
    far_values = far_rows(value_rows, flat_index)
    near_scores = jnp.einsum(
        "bqnhe,btnhe->bnhqt", query_blocks, near_keys, preferred_element_type=jnp.float32
    )
    far_scores = jnp.einsum(
        "bqnhe,nhbke->bnhqk", query_blocks, far_keys, preferred_element_type=jnp.float32
    )
    scores = jnp.where(
        key_mask, HDIM ** (-0.5) * jnp.concatenate([near_scores, far_scores], -1), MASKED
    )
    return (query_blocks, near_keys, near_values, far_keys, far_values, flat_index, scores)


def attend(queries, key_rows, value_rows, chosen_now, seq_start, seq_first):
    query_blocks, near_keys, near_values, far_keys, far_values, flat_index, scores = (
        attention_setup(queries, key_rows, value_rows, chosen_now, seq_start, seq_first)
    )
    span = WIN + QB
    row_top = jnp.max(scores, -1, keepdims=True)
    exp_terms = jnp.exp(scores - row_top)
    row_total = jnp.sum(exp_terms, -1, keepdims=True)
    softmax_low = (exp_terms / row_total).astype(jnp.bfloat16)
    near_part = jnp.einsum(
        "bnhqt,btnhe->bqnhe",
        softmax_low[..., :span],
        near_values,
        preferred_element_type=jnp.float32,
    )
    far_part = jnp.einsum(
        "bnhqk,nhbke->bqnhe",
        softmax_low[..., span:],
        far_values,
        preferred_element_type=jnp.float32,
    )
    return ((near_part + far_part).reshape(queries.shape), row_top + jnp.log(row_total))


def spread_back(near_grad, far_grad, flat_index, seq_start, seq_first, total_rows):
    blocks, span, buckets, heads_local, head_size = near_grad.shape
    length_local = blocks * QB
    feature_width = heads_local * head_size
    segment = jnp.zeros((length_local + WIN, buckets, heads_local, head_size), jnp.float32)
    for offset_index in range(WIN // QB + 1):
        piece = near_grad[:, offset_index * QB : (offset_index + 1) * QB].reshape(
            length_local, buckets, heads_local, head_size
        )
        segment = segment.at[offset_index * QB : offset_index * QB + length_local].add(piece)
    full_rows = jnp.zeros((total_rows * buckets * heads_local, head_size), jnp.float32)
    full_rows = full_rows.at[flat_index.reshape(-1)].add(far_grad.reshape(-1, head_size))
    full_rows = full_rows.reshape(total_rows, buckets, feature_width)
    local_part = segment[WIN:].reshape(length_local, buckets, feature_width)
    earlier = jnp.where(seq_first, 0.0, segment[:WIN].reshape(WIN, buckets, feature_width))
    full_rows = lax.dynamic_update_slice_in_dim(
        full_rows,
        lax.dynamic_slice_in_dim(full_rows, seq_start, length_local, 0) + local_part,
        seq_start,
        0,
    )
    earlier_start = jnp.maximum(seq_start - WIN, 0)
    full_rows = lax.dynamic_update_slice_in_dim(
        full_rows,
        lax.dynamic_slice_in_dim(full_rows, earlier_start, WIN, 0) + earlier,
        earlier_start,
        0,
    )
    return full_rows


def attend_back(
    queries, key_rows, value_rows, chosen_now, seq_start, seq_first, log_total, grad_mixed
):
    query_blocks, near_keys, near_values, far_keys, far_values, flat_index, scores = (
        attention_setup(queries, key_rows, value_rows, chosen_now, seq_start, seq_first)
    )
    span = WIN + QB
    score_scale = HDIM ** (-0.5)
    grad_blocks = grad_mixed.reshape(query_blocks.shape)
    weights_full = jnp.exp(scores - log_total)
    softmax_low = weights_full.astype(jnp.bfloat16)
    grad_near_weights = jnp.einsum(
        "bqnhe,btnhe->bnhqt", grad_blocks, near_values, preferred_element_type=jnp.float32
    )
    grad_far_weights = jnp.einsum(
        "bqnhe,nhbke->bnhqk", grad_blocks, far_values, preferred_element_type=jnp.float32
    )
    grad_weights = jnp.concatenate([grad_near_weights, grad_far_weights], -1)
    row_dot = jnp.sum(weights_full * grad_weights, -1, keepdims=True)
    grad_scores = (weights_full * (grad_weights - row_dot)).astype(jnp.bfloat16)
    grad_near, grad_far = (grad_scores[..., :span], grad_scores[..., span:])
    grad_queries = score_scale * (
        jnp.einsum("bnhqt,btnhe->bqnhe", grad_near, near_keys, preferred_element_type=jnp.float32)
        + jnp.einsum("bnhqk,nhbke->bqnhe", grad_far, far_keys, preferred_element_type=jnp.float32)
    )
    near_key_grad = score_scale * jnp.einsum(
        "bnhqt,bqnhe->btnhe", grad_near, query_blocks, preferred_element_type=jnp.float32
    )
    far_key_grad = score_scale * jnp.einsum(
        "bnhqk,bqnhe->nhbke", grad_far, query_blocks, preferred_element_type=jnp.float32
    )
    near_value_grad = jnp.einsum(
        "bnhqt,bqnhe->btnhe",
        softmax_low[..., :span],
        grad_blocks,
        preferred_element_type=jnp.float32,
    )
    far_value_grad = jnp.einsum(
        "bnhqk,bqnhe->nhbke",
        softmax_low[..., span:],
        grad_blocks,
        preferred_element_type=jnp.float32,
    )
    total_rows = key_rows.shape[0]
    key_grad = spread_back(
        near_key_grad, far_key_grad, flat_index, seq_start, seq_first, total_rows
    )
    value_grad = spread_back(
        near_value_grad, far_value_grad, flat_index, seq_start, seq_first, total_rows
    )
    return (grad_queries.reshape(queries.shape), key_grad, value_grad)


def forward_pass(hidden, params, chosen_now, query_mask, seq_start, seq_first, finish):
    (
        ln1_gain,
        ln1_shift,
        w_qkv,
        b_qv,
        w_out,
        b_out,
        ln2_gain,
        ln2_shift,
        w_fc,
        b_fc,
        w_proj,
        b_proj,
    ) = params
    hidden_wide = hidden.astype(jnp.float32)
    normed_all = gather_rows(layer_norm(hidden_wide, ln1_gain, ln1_shift).astype(jnp.bfloat16))
    projected = jnp.einsum("pnd,jdc->jpnc", normed_all, w_qkv, preferred_element_type=jnp.float32)
    queries = (projected[0] + b_qv[0]).astype(jnp.bfloat16)
    key_rows, value_rows = (
        lax.all_gather(projected[1].astype(jnp.bfloat16), "seq", axis=0, tiled=True),
        lax.all_gather((projected[2] + b_qv[1]).astype(jnp.bfloat16), "seq", axis=0, tiled=True),
    )
    attended, log_total = attend(queries, key_rows, value_rows, chosen_now, seq_start, seq_first)
    mixed_rows = (attended * query_mask[:, :, None]).astype(jnp.bfloat16)
    middle = hidden_wide + scatter_product(mixed_rows, w_out, "pnc,cd->pnd") + b_out
    normed_mlp = gather_rows(layer_norm(middle, ln2_gain, ln2_shift).astype(jnp.bfloat16))
    pre_active = (
        jnp.einsum("pnd,df->pnf", normed_mlp, w_fc, preferred_element_type=jnp.float32) + b_fc
    )
    active = gelu_tanh(pre_active).astype(jnp.bfloat16)
    if not finish:
        return (
            normed_all,
            queries,
            key_rows,
            value_rows,
            log_total,
            mixed_rows,
            middle,
            normed_mlp,
            pre_active,
            active,
        )
    output = (middle + scatter_product(active, w_proj, "pnf,fd->pnd") + b_proj).astype(jnp.bfloat16)
    return (output, (key_rows, value_rows))


def backward_pass(hidden, upstream, params, chosen_now, query_mask, seq_start, seq_first):
    (
        ln1_gain,
        ln1_shift,
        w_qkv,
        b_qv,
        w_out,
        b_out,
        ln2_gain,
        ln2_shift,
        w_fc,
        b_fc,
        w_proj,
        b_proj,
    ) = params
    (
        normed_all,
        queries,
        key_rows,
        value_rows,
        log_total,
        mixed_rows,
        middle,
        normed_mlp,
        pre_active,
        active,
    ) = forward_pass(hidden, params, chosen_now, query_mask, seq_start, seq_first, False)
    upstream_all = gather_rows(upstream)
    grad_w_proj = jnp.einsum(
        "pnf,pnd->fd", active, upstream_all, preferred_element_type=jnp.float32
    )
    grad_b_proj = jnp.sum(upstream.astype(jnp.float32), axis=(0, 1))
    grad_active = jnp.einsum(
        "pnd,fd->pnf", upstream_all, w_proj, preferred_element_type=jnp.float32
    )
    unused_value, gelu_pull = jax.vjp(gelu_tanh, pre_active)
    grad_pre = gelu_pull(grad_active)[0].astype(jnp.bfloat16)
    grad_w_fc = jnp.einsum("pnd,pnf->df", normed_mlp, grad_pre, preferred_element_type=jnp.float32)
    grad_b_fc = jnp.sum(grad_pre.astype(jnp.float32), axis=(0, 1))
    grad_normed_mlp = scatter_product(grad_pre, w_fc, "pnf,df->pnd")
    unused_norm, second_pull = jax.vjp(layer_norm, middle, ln2_gain, ln2_shift)
    grad_mid_norm, grad_ln2_gain, grad_ln2_shift = second_pull(grad_normed_mlp)
    grad_middle = upstream.astype(jnp.float32) + grad_mid_norm
    grad_branch = grad_middle.astype(jnp.bfloat16)
    grad_b_out = jnp.sum(grad_branch.astype(jnp.float32), axis=(0, 1))
    branch_all = gather_rows(grad_branch)
    grad_w_out = jnp.einsum(
        "pnc,pnd->cd", mixed_rows, branch_all, preferred_element_type=jnp.float32
    )
    grad_mixed = jnp.einsum(
        "pnd,cd->pnc", branch_all, w_out, preferred_element_type=jnp.float32
    ).astype(jnp.bfloat16) * query_mask[:, :, None].astype(jnp.bfloat16)
    grad_queries, key_grad_all, value_grad_all = attend_back(
        queries, key_rows, value_rows, chosen_now, seq_start, seq_first, log_total, grad_mixed
    )
    key_grad, value_grad = (
        lax.psum_scatter(
            key_grad_all.astype(jnp.bfloat16), "seq", scatter_dimension=0, tiled=True
        ).astype(jnp.float32),
        lax.psum_scatter(
            value_grad_all.astype(jnp.bfloat16), "seq", scatter_dimension=0, tiled=True
        ).astype(jnp.float32),
    )
    grad_project = jnp.stack(
        [
            grad_queries.astype(jnp.bfloat16),
            key_grad.astype(jnp.bfloat16),
            value_grad.astype(jnp.bfloat16),
        ],
        2,
    )
    grad_w_qkv = jnp.einsum(
        "pnd,pnjc->jdc", normed_all, grad_project, preferred_element_type=jnp.float32
    )
    grad_b_qv = jnp.sum(grad_project[:, :, 0::2].astype(jnp.float32), axis=(0, 1))
    grad_normed = scatter_product(grad_project, w_qkv, "pnjc,jdc->pnd")
    unused_first, first_pull = jax.vjp(layer_norm, hidden.astype(jnp.float32), ln1_gain, ln1_shift)
    grad_in_norm, grad_ln1_gain, grad_ln1_shift = first_pull(grad_normed)
    grad_hidden = (grad_middle + grad_in_norm).astype(jnp.bfloat16)
    block_grads = (
        grad_ln1_gain,
        grad_ln1_shift,
        grad_w_qkv,
        grad_b_qv,
        grad_w_out,
        grad_b_out,
        grad_ln2_gain,
        grad_ln2_shift,
        grad_w_fc,
        grad_b_fc,
        grad_w_proj,
        grad_b_proj,
    )
    return (grad_hidden, block_grads)


def on_device(
    inputs,
    cotangent,
    lengths,
    chosen,
    ln1_gain,
    ln1_shift,
    w_qkv,
    b_qv,
    w_out,
    b_out,
    ln2_gain,
    ln2_shift,
    w_fc,
    b_fc,
    w_proj,
    b_proj,
):
    params = tuple(
        (
            weight_array[0]
            for weight_array in (
                ln1_gain,
                ln1_shift,
                w_qkv,
                b_qv,
                w_out,
                b_out,
                ln2_gain,
                ln2_shift,
                w_fc,
                b_fc,
                w_proj,
                b_proj,
            )
        )
    )
    section_index = lax.axis_index("section")
    section_count = lax.axis_size("section")
    seq_index = lax.axis_index("seq")
    tensor_index = lax.axis_index("tensor")
    tensor_count = lax.axis_size("tensor")
    micro_count, rows_local, buckets, feature_width = inputs.shape
    length_local = rows_local * tensor_count
    heads_width = w_qkv.shape[-1]
    seq_start = seq_index * length_local
    seq_first = seq_index == 0
    positions = seq_start + lax.broadcasted_iota(jnp.int32, (micro_count, length_local, buckets), 1)
    mask_all = (positions < lengths[:, None, :]).astype(jnp.float32)
    mask_rows = lax.dynamic_slice_in_dim(mask_all, tensor_index * rows_local, rows_local, 1)
    step_count = micro_count + section_count - 1
    chosen_section = chosen[0]
    received = jnp.zeros((rows_local, buckets, feature_width), jnp.bfloat16)
    stored = jnp.zeros((micro_count, rows_local, buckets, feature_width), jnp.bfloat16)
    outputs = jnp.zeros_like(stored)
    for step_index in range(step_count):
        micro_index = step_index - section_index
        running = (micro_index >= 0) & (micro_index < micro_count)
        slot_index = jnp.clip(micro_index, 0, micro_count - 1)
        block_in = jnp.where(
            section_index == 0, lax.dynamic_index_in_dim(inputs, slot_index, 0, False), received
        )
        chosen_now = lax.dynamic_index_in_dim(chosen_section, slot_index, 0, False)
        query_mask = lax.dynamic_index_in_dim(mask_all, slot_index, 0, False)
        result, key_pair = forward_pass(
            block_in, params, chosen_now, query_mask, seq_start, seq_first, True
        )
        stored = jnp.where(
            running, lax.dynamic_update_index_in_dim(stored, block_in, slot_index, 0), stored
        )
        outputs = jnp.where(
            running, lax.dynamic_update_index_in_dim(outputs, result, slot_index, 0), outputs
        )
        received = from_behind(result, "section", 1)
    back_received = jnp.zeros((rows_local, buckets, feature_width), jnp.bfloat16)
    in_grads = jnp.zeros_like(stored)
    totals = None
    for step_index in range(step_count):
        micro_index = step_index - (section_count - 1 - section_index)
        running = (micro_index >= 0) & (micro_index < micro_count)
        slot_index = jnp.clip(micro_index, 0, micro_count - 1)
        chosen_now = lax.dynamic_index_in_dim(chosen_section, slot_index, 0, False)
        query_mask = lax.dynamic_index_in_dim(mask_all, slot_index, 0, False)
        local_mask = lax.dynamic_index_in_dim(mask_rows, slot_index, 0, False)
        top_grad = (
            lax.dynamic_index_in_dim(cotangent, slot_index, 0, False).astype(jnp.float32)
            * local_mask[:, :, None]
        ).astype(jnp.bfloat16)
        upstream = jnp.where(section_index == section_count - 1, top_grad, back_received)
        hidden = lax.dynamic_index_in_dim(stored, slot_index, 0, False)
        grad_hidden, block_grads = backward_pass(
            hidden, upstream, params, chosen_now, query_mask, seq_start, seq_first
        )
        block_grads = tuple(
            (jnp.where(running, grad_part, jnp.zeros_like(grad_part)) for grad_part in block_grads)
        )
        totals = (
            block_grads
            if step_index == 0
            else tuple(
                (total_part + grad_part for total_part, grad_part in zip(totals, block_grads))
            )
        )
        in_grads = jnp.where(
            running, lax.dynamic_update_index_in_dim(in_grads, grad_hidden, slot_index, 0), in_grads
        )
        back_received = from_behind(grad_hidden, "section", -1)
    (
        sum_ln1_gain,
        sum_ln1_shift,
        sum_w_qkv,
        sum_b_qv,
        sum_w_out,
        sum_b_out,
        sum_ln2_gain,
        sum_ln2_shift,
        sum_w_fc,
        sum_b_fc,
        sum_w_proj,
        sum_b_proj,
    ) = totals
    part_qkv, part_out, part_fc, part_proj = (
        lax.psum_scatter(
            sum_w_qkv.astype(jnp.bfloat16), "seq", scatter_dimension=1, tiled=True
        ).astype(jnp.float32),
        lax.psum_scatter(
            sum_w_out.astype(jnp.bfloat16), "seq", scatter_dimension=1, tiled=True
        ).astype(jnp.float32),
        lax.psum_scatter(
            sum_w_fc.astype(jnp.bfloat16), "seq", scatter_dimension=0, tiled=True
        ).astype(jnp.float32),
        lax.psum_scatter(
            sum_w_proj.astype(jnp.bfloat16), "seq", scatter_dimension=1, tiled=True
        ).astype(jnp.float32),
    )
    bias_qv = lax.dynamic_update_slice_in_dim(
        jnp.zeros((2, feature_width), jnp.float32), sum_b_qv, tensor_index * heads_width, 1
    )
    units_local = sum_b_fc.shape[0]
    bias_fc = lax.dynamic_update_slice_in_dim(
        jnp.zeros((units_local * tensor_count,), jnp.float32),
        sum_b_fc,
        tensor_index * units_local,
        0,
    )
    small_sums = lax.psum(
        (
            sum_ln1_gain,
            sum_ln1_shift,
            bias_qv,
            sum_b_out,
            sum_ln2_gain,
            sum_ln2_shift,
            bias_fc,
            sum_b_proj,
        ),
        ("seq", "tensor"),
    )
    return (
        outputs[None],
        in_grads[None],
        small_sums[0][None],
        small_sums[1][None],
        part_qkv[None],
        small_sums[2][None],
        part_out[None],
        small_sums[3][None],
        small_sums[4][None],
        small_sums[5][None],
        part_fc[None],
        small_sums[6][None],
        part_proj[None],
        small_sums[7][None],
    )


STREAMS = 4
NRM, NMLP, UPS, BRN, ACT, GPRE, MIX, DQKV = range(8)
F32 = jnp.float32
LOW = jnp.bfloat16
MESH_ID = pl.DeviceIdType.MESH


def dot_nn(left, right):
    return lax.dot_general(left, right, (((1,), (0,)), ((), ())), preferred_element_type=F32)


def dot_nt(left, right):
    return lax.dot_general(left, right, (((1,), (1,)), ((), ())), preferred_element_type=F32)


def dot_tn(left, right):
    return lax.dot_general(left, right, (((0,), (0,)), ((), ())), preferred_element_type=F32)


def standard(rows):
    centred = rows - jnp.mean(rows, axis=-1, keepdims=True)
    scale = lax.rsqrt(jnp.mean(centred * centred, axis=-1, keepdims=True) + NORM_EPS)
    return centred * scale, scale


def standard_back(grad, xhat, scale):
    inner = jnp.mean(grad * xhat, axis=-1, keepdims=True)
    return scale * (grad - jnp.mean(grad, axis=-1, keepdims=True) - xhat * inner)


def column_sum(rows):
    return jnp.sum(rows.astype(F32), axis=0, keepdims=True)


def relay_kernel(names, *refs):
    r = types.SimpleNamespace(**dict(zip(names, refs)))
    a, c, t = (lax.axis_index(name) for name in ("section", "seq", "tensor"))
    lines = lax.axis_size("section")
    chips = lax.axis_size("tensor")
    rows, buckets, width = r.inputs.shape[1:]
    half_width = width // 2
    local = rows * chips
    total = 2 * local
    stream_rows = local // STREAMS
    head_width = r.wo_in.shape[0]
    heads = head_width // HDIM
    blocks = local // QB
    units = r.wp_in.shape[0]
    scale = HDIM ** (-0.5)
    streams = range(STREAMS)

    def each_stream(*stages):
        def body(j, _):
            for stage in stages:
                stage(j)
            return 0

        lax.fori_loop(0, STREAMS, body, 0)

    def remote(src, dst, send, recv, **target):
        return pltpu.make_async_remote_copy(
            src_ref=src,
            dst_ref=dst,
            send_sem=send,
            recv_sem=recv,
            device_id=target,
            device_id_type=MESH_ID,
        )

    def drain(ref, sem):
        pltpu.make_async_copy(ref, ref, sem).wait()

    def row_block(index, size):
        return pl.ds(pl.multiple_of(index * size, size), size)

    near_chip = t + 1 - 2 * (t % 2)
    over_chip = (t + 2) % 4
    across_chip = 3 - t
    middle_chip = (t == 1) | (t == 2)
    end_chip = (t == 0) | (t == 3)
    owned = stream_rows // 2
    mine = row_block(t - 1, owned)
    my_half = row_block(c, local)

    barrier = pltpu.get_barrier_semaphore()
    for core in range(2):
        for step in range(1, chips):
            there = {"tensor": (t + step) % chips, "seq": core}
            pl.semaphore_signal(barrier, inc=1, device_id=there, device_id_type=MESH_ID)
        for step in range(1, lines):
            there = {"section": (a + step) % lines, "seq": core}
            pl.semaphore_signal(barrier, inc=1, device_id=there, device_id_type=MESH_ID)
    for step in range(1, lines):
        there = {"section": (a + step) % lines, "tensor": near_chip}
        pl.semaphore_signal(barrier, inc=1, device_id=there, device_id_type=MESH_ID)
    pl.semaphore_signal(barrier, inc=1, device_id={"seq": 1 - c}, device_id_type=MESH_ID)
    pl.semaphore_wait(barrier, 2 * (chips - 1) + 3 * (lines - 1) + 1)

    def beside(s):
        return s + 1 - 2 * (s % 2)

    def above(s):
        return (s + 2) % 4

    def store(p):
        return (r.wq, r.wo, r.wf, r.wp)[p]

    def source(p):
        return (r.wq_in, r.wo_in, r.wf_in, r.wp_in)[p]

    def height(p):
        return source(p).shape[0]

    def core_half(p, s, core):
        return store(p).at[s, row_block(core, height(p) // 2)]

    def first_hop(p, s, neighbour, which):
        return remote(
            source(p).at[row_block(c, height(p) // 2)],
            core_half(p, s, c),
            r.w_first_s.at[p, which],
            r.w_first_r.at[s, p],
            section=neighbour,
        )

    def second_hop(p, s, which):
        view = store(p).at[s, row_block(2 * c + which, height(p) // 4)]
        return remote(
            view, view, r.w_second_s.at[s, p], r.w_second_r.at[s, p, which], section=3 - s
        )

    def core_hop(p, s, core):
        view = core_half(p, s, core)
        return remote(view, view, r.w_core_s.at[s, p], r.w_core_r.at[s, p], seq=1 - c)

    def own_copy(p):
        return pltpu.make_async_copy(source(p), store(p).at[a], r.w_own.at[p])

    def pass_on(s, p, which):
        line = (beside(s), above(s))[which]

        @pl.when(a == line)
        def _():
            first_hop(p, s, line, which).wait_recv()
            second_hop(p, s, which).start()
            core_hop(p, s, c).start()

    def pass_all(s, pieces):
        for p in pieces:
            for which in range(2):
                pass_on(s, p, which)

    def pass_far(s, p):
        @pl.when(a == 3 - s)
        def _():
            second_hop(p, s, 0).wait_recv()
            second_hop(p, s, 1).wait_recv()
            core_hop(p, s, c).start()

    def need(s, p):
        @pl.when(s == 0)
        def _():
            if p < 2:
                pass_all(0, (p,))
            pass_far(0, p)

        @pl.when(a == s)
        def _():
            own_copy(p).wait()

        @pl.when(a != s)
        def _():
            core_hop(p, s, 1 - c).wait_recv()

    def small_copy(step, line, slot):
        return remote(
            r.small_own, r.small.at[slot], r.small_s.at[step], r.small_r.at[slot], section=line
        )

    def count_copy(step, line, slot):
        return remote(
            r.count_own.at[line],
            r.count.at[slot],
            r.count_s.at[step],
            r.count_r.at[slot],
            section=line,
        )

    singles = (r.ln1_gain, r.ln1_shift, r.ln2_gain, r.ln2_shift, r.b_out, r.b_proj)
    for place, single in enumerate(singles):
        r.small_own[place : place + 1] = single[...]
    r.small_own[6:7, :units] = r.b_fc[...]
    r.small_own[7:8, :head_width] = r.b_qv[0:1]
    r.small_own[7:8, half_width : half_width + head_width] = r.b_qv[1:2]
    for step in range(1, lines):
        small_copy(step - 1, (a + step) % lines, a).start()
    for p in range(4):
        for which, line in enumerate((beside(a), above(a))):
            first_hop(p, a, line, which).start()
    for p in range(4):
        own_copy(p).start()
    r.small[a] = r.small_own[...]

    def place_of(index):
        inside = index % local
        stream, left = inside // stream_rows, inside % stream_rows
        first = (index // local) * local + (left // owned) * (local // 2)
        return first + stream * owned + left % owned

    def iota(shape, dimension):
        return lax.broadcasted_iota(jnp.int32, shape, dimension)

    square = jnp.where(iota((KSEL, KSEL), 0) == iota((KSEL, KSEL), 1), 1.0, 0.0).astype(LOW)
    position = place_of(iota((KSEL, total), 1)).astype(F32)
    for pair in range(lines * heads):
        line, head = pair // heads, pair % heads
        columns = dot_nt(square, r.chosen[pair].astype(F32).astype(LOW))
        for block in range(blocks):
            pick = head * blocks + block
            r.count_own[line, pick : pick + 1, :] = jnp.sum(
                jnp.where(columns[:, block : block + 1] == position, 1.0, 0.0),
                axis=0,
                keepdims=True,
            )
    for step in range(1, lines):
        count_copy(step - 1, (a + step) % lines, a).start()
    r.count[a] = r.count_own[a]

    NEAR, OVER, ACROSS = range(3)

    def gather(buffer, s, kind, j, owner, target, slot):
        view = buffer.at[s, j, row_block(owner - 1, owned)]
        return remote(
            view, view, r.ag_s.at[kind, j, slot], r.ag_r.at[kind, j, slot], tensor=target
        )

    def used_before(s, kind):
        return s > 0 if kind < 2 else s < lines - 1

    def gather_start(buffer, s, kind, j):
        @pl.when(used_before(s, kind))
        def _():
            gather_sent(buffer, s, kind, j)

        gather(buffer, s, kind, j, t, over_chip, OVER).start()
        gather(buffer, s, kind, j, t, across_chip, ACROSS).start()
        gather(buffer, s, kind, j, t, near_chip, NEAR).start()

    def gather_wait(buffer, s, kind, j):
        @pl.when(middle_chip)
        def _():
            gather(buffer, s, kind, j, across_chip, across_chip, ACROSS).wait_recv()

        @pl.when(end_chip)
        def _():
            gather(buffer, s, kind, j, near_chip, near_chip, NEAR).wait_recv()
            gather(buffer, s, kind, j, over_chip, over_chip, OVER).wait_recv()

    def gather_sent(buffer, s, kind, j):
        gather(buffer, s, kind, j, t, over_chip, OVER).wait_send()
        gather(buffer, s, kind, j, t, across_chip, ACROSS).wait_send()
        gather(buffer, s, kind, j, t, near_chip, NEAR).wait_send()

    def scatter(s, kind, j, owner, slot):
        return remote(
            r.part.at[kind, j, row_block(owner - 1, owned)],
            r.arrived.at[s, kind, j, slot],
            r.rs_s.at[kind, j, slot],
            r.rs_r.at[kind, j, slot],
            tensor=owner,
        )

    def scatter_start(s, kind, j, product):
        @pl.when(used_before(s, kind))
        def _():
            scatter_sent(s, kind, j)

        r.part[kind, j] = product.astype(LOW)

        @pl.when(end_chip)
        def _():
            scatter(s, kind, j, over_chip, OVER).start()
            scatter(s, kind, j, near_chip, NEAR).start()

        @pl.when(middle_chip)
        def _():
            scatter(s, kind, j, across_chip, ACROSS).start()

    def scatter_sum(s, kind, j):
        result = r.part[kind, j, mine].astype(F32)
        for slot in (NEAR, ACROSS, OVER):
            scatter(s, kind, j, t, slot).wait_recv()
            result = result + r.arrived[s, kind, j, slot].astype(F32)
        return result

    def scatter_sent(s, kind, j):
        @pl.when(end_chip)
        def _():
            scatter(s, kind, j, over_chip, OVER).wait_send()
            scatter(s, kind, j, near_chip, NEAR).wait_send()

        @pl.when(middle_chip)
        def _():
            scatter(s, kind, j, across_chip, ACROSS).wait_send()

    own_rows = (r.nrm, r.nmlp, r.ups, r.brn, r.act, r.gpre, r.mix, r.dqkv)
    all_rows = (
        r.all_nrm,
        r.all_nmlp,
        r.all_ups,
        r.all_brn,
        r.all_act,
        r.all_gpre,
        r.all_mix,
        r.all_dqkv,
    )

    def rows_copy(index, s, same, stays=False):
        core = c if same else 1 - c
        src = own_rows[index].at[s]
        dst = all_rows[index].at[a, c]
        if index <= BRN:
            src = src.at[:, :, row_block(core, half_width)]
        recv = r.rows_r.at[index]
        if stays:
            return pltpu.make_async_copy(src, dst, recv)
        if same:
            return remote(src, dst, r.rows_s.at[index, s, 0], recv, section=s)
        return remote(src, dst, r.rows_s.at[index, s, 1], recv, section=s, seq=1 - c)

    def rows_start(index, s):
        @pl.when(a == s)
        def _():
            rows_copy(index, s, True, True).start()

        @pl.when(a != s)
        def _():
            rows_copy(index, s, True).start()

        if index <= BRN:
            rows_copy(index, s, False).start()

    def forward_rows(s):
        for index in (NRM, MIX, NMLP, ACT):
            rows_start(index, s)

    def rows_sent(index, s):
        @pl.when(a != s)
        def _():
            rows_copy(index, s, True).wait_send()

        if index <= BRN:
            rows_copy(index, s, False).wait_send()

    def share_copy(index, core):
        view = all_rows[index].at[:, core]
        return remote(view, view, r.share_s.at[index - ACT], r.share_r.at[index - ACT], seq=1 - c)

    def share(index):
        drain(all_rows[index].at[:, c], r.rows_r.at[index])
        share_copy(index, c).start()

    def norm_copy(s):
        return remote(
            r.norm_part.at[s], r.norm_all.at[a], r.norm_s.at[s], r.norm_r, section=s
        )

    def norm_start(s):
        @pl.when(a == s)
        def _():
            pltpu.make_async_copy(r.norm_part.at[s], r.norm_all.at[a], r.norm_r).start()

        @pl.when(a != s)
        def _():
            norm_copy(s).start()

    def home_copy(what, s, chip):
        src, dst, send, recv = what
        return remote(
            src.at[s, chip % 2],
            dst.at[a],
            send.at[s, chip % 2],
            recv,
            section=s,
            tensor=chip,
        )

    def home_start(what, s):
        src, dst, send, recv = what

        @pl.when(middle_chip & (a == s))
        def _():
            pltpu.make_async_copy(src.at[s, t % 2], dst.at[a], recv).start()

        @pl.when(middle_chip & (a != s))
        def _():
            home_copy(what, s, t).start()

        @pl.when(middle_chip)
        def _():
            home_copy(what, s, near_chip).start()

    def home_sent(what, s):
        @pl.when(middle_chip & (a != s))
        def _():
            home_copy(what, s, t).wait_send()

        @pl.when(middle_chip)
        def _():
            home_copy(what, s, near_chip).wait_send()

    out_home = (r.out_low, r.acts, r.out_s, r.out_r)
    grad_home = (r.grad_low, r.grads, r.grad_s, r.grad_r)

    length = r.lengths[a // buckets, a % buckets]
    key = place_of(iota((stream_rows, total), 1))
    for j in streams:
        query = place_of(c * local + j * stream_rows + iota((stream_rows, total), 0))
        r.near[j] = jnp.where((query >= key) & (query - key < WIN), 1.0, 0.0)
    key_row = place_of(iota((1, total), 1))

    def row_mask(place):
        return jnp.where(place < length, 1.0, 0.0)

    def multiplicity(s, j, head):
        far = []
        for block in range(blocks):
            pick = head * blocks + block
            limit = (c * blocks + block) * QB - WIN
            counted = jnp.where(key_row <= limit, r.count[s, pick : pick + 1, :], 0.0)
            far.append(jnp.broadcast_to(counted, (stream_rows // blocks, total)))
        return r.near[j] + jnp.concatenate(far, axis=0)

    def head_cols(head):
        return slice(head * HDIM, (head + 1) * HDIM)

    def kv_copy(s):
        view = r.kv.at[s, :, 0:local]
        return remote(view, view, r.kv_s.at[s], r.kv_r.at[s], seq=1 - c)

    def dkv_copy(s):
        return remote(r.dkv_out.at[s], r.dkv_in.at[s], r.dkv_s.at[s], r.dkv_r.at[s], seq=1 - c)

    def own_sequence(ref):
        both = ref[a // buckets].astype(F32)
        picked = both[:, 0, :]
        for bucket in range(1, buckets):
            picked = jnp.where(a % buckets == bucket, both[:, bucket, :], picked)
        return picked

    def own_part(j):
        chip, first = (j * owned) // rows, (j * owned) % rows
        return chip, slice(first, first + owned)

    def first_copy():
        return remote(r.first_out, r.first_in, r.first_s, r.first_r, tensor=near_chip)

    own_place = c * local + t * rows + iota((rows, 1), 0)
    r.first_out[0] = own_sequence(r.inputs).astype(LOW)
    r.first_out[1] = (own_sequence(r.cotangent) * row_mask(own_place)).astype(LOW)
    r.norm_part[...] = jnp.zeros_like(r.norm_part)

    @pl.when(c == 0)
    def _():
        r.kv[:, :, local:total] = jnp.zeros((lines, 2, local, head_width), LOW)


    @pl.when(end_chip)
    def _():
        first_copy().start()

    @pl.when(middle_chip)
    def _():
        first_copy().wait_recv()
        for which in range(2):
            here, beside_it = r.first_out[which].astype(F32), r.first_in[which].astype(F32)
            lower = jnp.where(t % 2 == 0, here, beside_it)
            upper = jnp.where(t % 2 == 0, beside_it, here)
            for j in streams:
                chip, part = own_part(j)
                own_block = (lower, upper)[chip][part]
                if which == 0:
                    r.hidden[j] = own_block
                else:
                    r.upstream[j] = own_block.astype(LOW)

    def on_owner(stage):
        def run(s, j):
            @pl.when(middle_chip)
            def _():
                stage(s, j)

        return run

    def keep_rows(target, s, j, result):
        place = row_block(j % (rows // owned), owned)
        target[s, (j * owned) // rows, place] = result

    @on_owner
    def enter(s, j):
        xhat, inverse = standard(r.hidden[j])
        r.xhat1[s, j] = xhat
        r.inv1[s, j] = jnp.broadcast_to(inverse, (owned, 128))
        r.nrm[s, j, mine] = (xhat * r.small[s, 0:1] + r.small[s, 1:2]).astype(LOW)
        gather_start(r.nrm, s, 0, j)

    def project(s, j):
        gather_wait(r.nrm, s, 0, j)
        normed = r.nrm[s, j]
        place = row_block(c * STREAMS + j, stream_rows)
        bias_v = r.small[s, 7:8, half_width : half_width + head_width]
        key_rows = dot_nt(normed, r.wq[s, head_width : 2 * head_width])
        value_rows = dot_nt(normed, r.wq[s, 2 * head_width : 3 * head_width]) + bias_v
        r.kv[s, 0, place] = key_rows.astype(LOW)
        r.kv[s, 1, place] = value_rows.astype(LOW)

    def ask(s, j):
        queries = dot_nt(r.nrm[s, j], r.wq[s, 0:head_width]) + r.small[s, 7:8, :head_width]
        r.qry[s, j] = queries.astype(LOW)

    def attend_line(s, j):
        mixed = []
        for head in range(heads):
            cols = head_cols(head)
            times = multiplicity(s, j, head)
            scores = scale * dot_nt(r.qry[s, j, :, cols], r.kv[s, 0, :, cols])
            scores = jnp.where(times > 0.0, scores, MASKED)
            top = jnp.max(scores, axis=-1, keepdims=True)
            terms = times * jnp.exp(scores - top)
            weights = terms / jnp.sum(terms, axis=-1, keepdims=True)
            r.soft[s, j, head] = weights
            mixed.append(dot_nn(weights.astype(LOW), r.kv[s, 1, :, cols]))
        mask = row_mask(place_of(c * local + j * stream_rows + iota((stream_rows, 1), 0)))
        r.mix[s, j] = (jnp.concatenate(mixed, axis=-1) * mask).astype(LOW)

    def leave_attention(s, j):
        scatter_start(s, 0, j, dot_nn(r.mix[s, j], r.wo[s]))

    @on_owner
    def between(s, j):
        middle = r.hidden[j] + scatter_sum(s, 0, j) + r.small[s, 4:5]
        r.middle[j] = middle
        xhat, inverse = standard(middle)
        r.xhat2[s, j] = xhat
        r.inv2[s, j] = jnp.broadcast_to(inverse, (owned, 128))
        r.nmlp[s, j, mine] = (xhat * r.small[s, 2:3] + r.small[s, 3:4]).astype(LOW)
        gather_start(r.nmlp, s, 1, j)

    def feed(s, j):
        gather_wait(r.nmlp, s, 1, j)
        before = dot_nn(r.nmlp[s, j], r.wf[s]) + r.small[s, 6:7, :units]
        bend = jnp.tanh(0.7978845608028654 * (before + 0.044715 * before * before * before))
        r.act[s, j] = (0.5 * before * (1.0 + bend)).astype(LOW)
        r.slope[s, j] = 0.5 * (1.0 + bend) + 0.5 * before * (1.0 - bend * bend) * (
            0.7978845608028654 * (1.0 + 3 * 0.044715 * before * before)
        )


    def leave_feed(s, j):
        scatter_start(s, 1, j, dot_nn(r.act[s, j], r.wp[s]))

    @on_owner
    def finish(s, j):
        result = r.middle[j] + scatter_sum(s, 1, j) + r.small[s, 5:6]
        keep_rows(r.out_low, s, j, result.astype(LOW))
        r.hidden[j] = result.astype(LOW).astype(F32)

    def small_ready(s):
        @pl.when(a != s)
        def _():
            small_copy(0, a, s).wait_recv()

    small_ready(0)
    for j in streams:
        enter(0, j)

    def forward(s, _):
        need(s, 0)
        each_stream(lambda j: project(s, j))

        @pl.when(c == 0)
        def _():
            kv_copy(s).start()

        each_stream(lambda j: ask(s, j))

        @pl.when(a != s)
        def _():
            count_copy(0, a, s).wait_recv()

        @pl.when(c == 1)
        def _():
            kv_copy(s).wait_recv()

        need(s, 1)
        each_stream(lambda j: attend_line(s, j), lambda j: leave_attention(s, j))

        @pl.when(s == 0)
        def _():
            pass_all(0, (2,))
            for later in range(1, lines):
                pass_all(later, (0, 1, 2))

        @pl.when(s == 1)
        def _():
            pass_far(1, 2)
            pass_far(1, 3)
            for later in range(2, lines):
                for p in range(4):
                    pass_far(later, p)

        each_stream(lambda j: between(s, j))
        @pl.when(s == 0)
        def _():
            for later in range(lines):
                pass_all(later, (3,))

        need(s, 2)
        need(s, 3)
        each_stream(lambda j: feed(s, j), lambda j: leave_feed(s, j))


        @pl.when(s >= 2)
        def _():
            forward_rows(s - 2)


        @pl.when(s + 1 < lines)
        def _():
            small_ready(s + 1)

        def go_on(j):
            @pl.when(s + 1 < lines)
            def _():
                enter(s + 1, j)

        each_stream(lambda j: finish(s, j), go_on)

        home_start(out_home, s)

        @pl.when(s == 0)
        def _():
            pass_far(1, 0)
            pass_far(1, 1)

        return 0

    lax.fori_loop(0, lines, forward, 0)

    @on_owner
    def turn(s, j):
        upstream = r.upstream[j]
        r.ups[s, j, mine] = upstream
        gather_start(r.ups, s, 2, j)
        r.norm_part[s, 5:6] += column_sum(upstream)

    def feed_back(s, j):
        gather_wait(r.ups, s, 2, j)
        grad_pre = (dot_nt(r.ups[s, j], r.wp[s]) * r.slope[s, j]).astype(LOW)
        r.gpre[s, j] = grad_pre
        scatter_start(s, 2, j, dot_nt(grad_pre, r.wf[s]))
        r.norm_part[s, 6:7, :units] += column_sum(grad_pre)

    @on_owner
    def between_back(s, j):
        grad = scatter_sum(s, 2, j)
        xhat = r.xhat2[s, j]
        upstream = r.upstream[j].astype(F32)
        grad_middle = upstream + standard_back(
            grad * r.small[s, 2:3], xhat, r.inv2[s, j, :, 0:1]
        )
        r.middle[j] = grad_middle
        branch = grad_middle.astype(LOW)
        r.brn[s, j, mine] = branch
        gather_start(r.brn, s, 3, j)
        r.norm_part[s, 2:3] += column_sum(grad * xhat)
        r.norm_part[s, 3:4] += column_sum(grad)
        r.norm_part[s, 4:5] += column_sum(branch)

    def mixed_back(s, j):
        gather_wait(r.brn, s, 3, j)
        place = place_of(c * local + j * stream_rows + iota((stream_rows, 1), 0))
        r.gmix[j] = (dot_nt(r.brn[s, j], r.wo[s]) * row_mask(place)).astype(LOW)

    def attend_line_back(s, j):
        grad_q, grad_k, grad_v = [], [], []
        for head in range(heads):
            cols = head_cols(head)
            weights = r.soft[s, j, head]
            grad_head = r.gmix[j, :, cols]
            grad_weights = dot_nt(grad_head, r.kv[s, 1, :, cols])
            inner = jnp.sum(weights * grad_weights, axis=-1, keepdims=True)
            grad_scores = (weights * (grad_weights - inner)).astype(LOW)
            grad_k.append(scale * dot_tn(grad_scores, r.qry[s, j, :, cols]))
            grad_v.append(dot_tn(weights.astype(LOW), grad_head))
            grad_q.append(scale * dot_nn(grad_scores, r.kv[s, 0, :, cols]))
        for which, grad in enumerate((grad_k, grad_v)):
            grad = jnp.concatenate(grad, axis=-1)
            r.dkv_all[which] += grad
        grad_q = jnp.concatenate(grad_q, axis=-1).astype(LOW)
        r.dqkv[s, 0, j] = grad_q
        r.norm_part[s, 7:8, :head_width] += column_sum(grad_q)

    def join_keys(s):
        @pl.when(c == 1)
        def _():
            r.dkv_out[s] = r.dkv_all[:, 0:local].astype(LOW)
            dkv_copy(s).start()

        @pl.when(c == 0)
        def _():
            dkv_copy(s).wait_recv()
            r.dkv_all[:, 0:local] += r.dkv_in[s].astype(F32)

        for which in range(2):
            joined = r.dkv_all[which, my_half].astype(LOW)
            r.dqkv[s, 1 + which] = joined.reshape(r.dqkv.shape[2:])
            if which == 1:
                r.norm_part[s, 7:8, half_width : half_width + head_width] = column_sum(joined)

    def leave_back(s, j):
        product = dot_nn(r.dqkv[s, 0, j], r.wq[s, 0:head_width])
        for which in range(1, 3):
            weight = r.wq[s, which * head_width : (which + 1) * head_width]
            product = product + dot_nn(r.dqkv[s, which, j], weight)
        scatter_start(s, 3, j, product)

    @on_owner
    def finish_back(s, j):
        grad = scatter_sum(s, 3, j)
        xhat = r.xhat1[s, j]
        result = r.middle[j] + standard_back(
            grad * r.small[s, 0:1], xhat, r.inv1[s, j, :, 0:1]
        )
        r.upstream[j] = result.astype(LOW)
        keep_rows(r.grad_low, s, j, result.astype(LOW))
        r.norm_part[s, 0:1] += column_sum(grad * xhat)
        r.norm_part[s, 1:2] += column_sum(grad)

    for j in streams:
        turn(lines - 1, j)

    def backward(index, _):
        s = lines - 1 - index
        each_stream(lambda j: feed_back(s, j))
        rows_start(UPS, s)
        rows_start(GPRE, s)

        @pl.when(index < 2)
        def _():
            forward_rows(lines - 2 + index)

        @pl.when(index == lines - 1)
        def _():
            share(ACT)
            share(MIX)

        each_stream(lambda j: between_back(s, j))
        r.dkv_all[...] = jnp.zeros(r.dkv_all.shape, F32)
        each_stream(lambda j: mixed_back(s, j), lambda j: attend_line_back(s, j))
        join_keys(s)
        rows_start(BRN, s)
        each_stream(lambda j: leave_back(s, j))
        rows_start(DQKV, s)
        def go_on(j):
            @pl.when(s > 0)
            def _():
                turn(s - 1, j)

        each_stream(lambda j: finish_back(s, j), go_on)

        norm_start(s)
        home_start(grad_home, s)
        return 0

    lax.fori_loop(0, lines, backward, 0)

    share(GPRE)
    share(DQKV)

    drain(r.norm_all, r.norm_r)
    slot = c * chips + t
    norm_sum = r.norm_all[0]
    for line in range(1, lines):
        norm_sum = norm_sum + r.norm_all[line]
    r.ends[slot] = norm_sum

    def ends_copy(step):
        core, chip = step // chips, step % chips
        view = r.ends.at[slot]
        return remote(
            view,
            view,
            r.ends_s.at[step - 1],
            r.ends_r,
            seq=(c + core) % 2,
            tensor=(t + chip) % chips,
        )

    for step in range(1, 2 * chips):
        ends_copy(step).start()

    for kind, buffer in enumerate((r.nrm, r.nmlp, r.ups, r.brn)):
        for j in streams:
            scatter_sent(0, kind, j)

            @pl.when(middle_chip)
            def _():
                gather_sent(buffer, 0, kind, j)

    for index in range(ACT):
        drain(all_rows[index], r.rows_r.at[index])
    for index in range(ACT, 8):
        share_copy(index, 1 - c).wait_recv()
        share_copy(index, c).wait_send()
    drain(r.acts, r.out_r)
    drain(r.grads, r.grad_r)
    drain(r.ends.at[0 : 2 * chips - 1], r.ends_r)
    for step in range(1, 2 * chips):
        ends_copy(step).wait_send()
    for step in range(1, lines):
        small_copy(step - 1, (a + step) % lines, a).wait_send()
        count_copy(step - 1, (a + step) % lines, a).wait_send()
    for p in range(4):
        for which, line in enumerate((beside(a), above(a))):
            first_hop(p, a, line, which).wait_send()

    @pl.when(end_chip)
    def _():
        first_copy().wait_send()

    def sent(s, _):
        home_sent(out_home, s)
        home_sent(grad_home, s)

        @pl.when(a != s)
        def _():
            norm_copy(s).wait_send()

        @pl.when(c == 0)
        def _():
            kv_copy(s).wait_send()

        @pl.when(c == 1)
        def _():
            dkv_copy(s).wait_send()

        for index in range(8):
            rows_sent(index, s)
        for p in range(4):

            @pl.when((a == beside(s)) | (a == above(s)))
            def _():
                second_hop(p, s, 0).wait_send()

            @pl.when(a != s)
            def _():
                core_hop(p, s, c).wait_send()

        return 0

    lax.fori_loop(0, lines, sent, 0)


def relay_call(inputs, cotangent, lengths, chosen, singles, weights):
    lines = lax.axis_size("section")
    chips = lax.axis_size("tensor")
    rows, buckets, width = inputs.shape[1:]
    local, total, half = rows * chips, 2 * rows * chips, width // 2
    head_width, units = weights["wo_in"].shape[0], weights["wp_in"].shape[0]
    heads = head_width // HDIM
    stream = local // STREAMS
    peers, owned = chips - 1, stream // 2
    vmem, dma = pltpu.VMEM, pltpu.SemaphoreType.DMA
    operands = dict(
        inputs=inputs,
        cotangent=cotangent,
        lengths=lengths,
        chosen=chosen,
        **singles,
        **weights,
    )

    def space(name):
        if name in weights:
            return pl.ANY
        return pltpu.SMEM if operands[name] is lengths else pltpu.VMEM

    sums = dict(
        acts=((lines, rows, width), LOW),
        grads=((lines, rows, width), LOW),
        ends=((2 * chips, 8, width), F32),
    )
    gathered = dict(
        all_nrm=((lines, 2, STREAMS, stream, half), LOW),
        all_nmlp=((lines, 2, STREAMS, stream, half), LOW),
        all_ups=((lines, 2, STREAMS, stream, half), LOW),
        all_brn=((lines, 2, STREAMS, stream, half), LOW),
        all_act=((lines, 2, STREAMS, stream, units), LOW),
        all_gpre=((lines, 2, STREAMS, stream, units), LOW),
        all_mix=((lines, 2, STREAMS, stream, head_width), LOW),
        all_dqkv=((lines, 2, 3, STREAMS, stream, head_width), LOW),
    )
    outputs = dict(**sums, **gathered)
    scratch = dict(
        wq=vmem((lines,) + weights["wq_in"].shape, LOW),
        wo=vmem((lines,) + weights["wo_in"].shape, LOW),
        wf=vmem((lines,) + weights["wf_in"].shape, LOW),
        wp=vmem((lines,) + weights["wp_in"].shape, LOW),
        small_own=vmem((8, width), F32),
        small=vmem((lines, 8, width), F32),
        count_own=vmem((lines, 8, total), F32),
        count=vmem((lines, 8, total), F32),
        hidden=vmem((STREAMS, owned, width), F32),
        middle=vmem((STREAMS, owned, width), F32),
        upstream=vmem((STREAMS, owned, width), LOW),
        first_out=vmem((2, rows, width), LOW),
        first_in=vmem((2, rows, width), LOW),
        xhat1=vmem((lines, STREAMS, owned, width), F32),
        inv1=vmem((lines, STREAMS, owned, 128), F32),
        xhat2=vmem((lines, STREAMS, owned, width), F32),
        inv2=vmem((lines, STREAMS, owned, 128), F32),
        nrm=vmem((lines, STREAMS, stream, width), LOW),
        nmlp=vmem((lines, STREAMS, stream, width), LOW),
        ups=vmem((lines, STREAMS, stream, width), LOW),
        brn=vmem((lines, STREAMS, stream, width), LOW),
        act=vmem((lines, STREAMS, stream, units), LOW),
        gpre=vmem((lines, STREAMS, stream, units), LOW),
        slope=vmem((lines, STREAMS, stream, units), F32),
        mix=vmem((lines, STREAMS, stream, head_width), LOW),
        qry=vmem((lines, STREAMS, stream, head_width), LOW),
        gmix=vmem((STREAMS, stream, head_width), LOW),
        dqkv=vmem((lines, 3, STREAMS, stream, head_width), LOW),
        kv=vmem((lines, 2, total, head_width), LOW),
        soft=vmem((lines, STREAMS, heads, stream, total), F32),
        near=vmem((STREAMS, stream, total), F32),
        dkv_all=vmem((2, total, head_width), F32),
        dkv_out=vmem((lines, 2, local, head_width), LOW),
        dkv_in=vmem((lines, 2, local, head_width), LOW),
        part=vmem((4, STREAMS, stream, width), LOW),
        arrived=vmem((lines, 4, STREAMS, peers, owned, width), LOW),
        out_low=vmem((lines, 2, rows, width), LOW),
        grad_low=vmem((lines, 2, rows, width), LOW),
        norm_part=vmem((lines, 8, width), F32),
        norm_all=vmem((lines, 8, width), F32),
        w_first_s=dma((4, 2)),
        w_first_r=dma((lines, 4)),
        w_second_s=dma((lines, 4)),
        w_second_r=dma((lines, 4, 2)),
        w_core_s=dma((lines, 4)),
        w_core_r=dma((lines, 4)),
        w_own=dma((4,)),
        small_s=dma((lines - 1,)),
        small_r=dma((lines,)),
        count_s=dma((lines - 1,)),
        count_r=dma((lines,)),
        ag_s=dma((4, STREAMS, peers)),
        ag_r=dma((4, STREAMS, peers)),
        rs_s=dma((4, STREAMS, peers)),
        rs_r=dma((4, STREAMS, peers)),
        kv_s=dma((lines,)),
        kv_r=dma((lines,)),
        dkv_s=dma((lines,)),
        dkv_r=dma((lines,)),
        rows_s=dma((8, lines, 2)),
        rows_r=dma((8,)),
        share_s=dma((4,)),
        share_r=dma((4,)),
        first_s=dma,
        first_r=dma,
        out_s=dma((lines, 2)),
        out_r=dma,
        grad_s=dma((lines, 2)),
        grad_r=dma,
        norm_s=dma((lines,)),
        norm_r=dma,
        ends_s=dma((2 * chips - 1,)),
        ends_r=dma,
    )
    names = tuple(operands) + tuple(outputs) + tuple(scratch)
    results = pl.pallas_call(
        functools.partial(relay_kernel, names),
        out_shape=[jax.ShapeDtypeStruct(shape, kind) for shape, kind in outputs.values()],
        in_specs=[pl.BlockSpec(memory_space=space(name)) for name in operands],
        out_specs=[
            pl.BlockSpec(memory_space=pl.ANY if name in gathered else pltpu.VMEM)
            for name in outputs
        ],
        scratch_shapes=list(scratch.values()),
        compiler_params=pltpu.CompilerParams(
            collective_id=0, has_side_effects=True, vmem_limit_bytes=60 * 2**20
        ),
        name="relay",
    )(*operands.values())
    return dict(zip(outputs, results))


def weights_kernel(names, *refs):
    r = types.SimpleNamespace(**dict(zip(names, refs)))
    step = pl.program_id(0)
    micro_count, rows, buckets, width = r.activations.shape
    chips, units, head_width = r.ends.shape[0] // 2, r.all_act.shape[-1], r.all_mix.shape[-1]

    @pl.when(step == 0)
    def _():
        sums = r.ends[0]
        for other in range(1, 2 * chips):
            sums = sums + r.ends[other]
        singles = (r.ln1_gain, r.ln1_shift, r.ln2_gain, r.ln2_shift, r.b_out, r.b_proj)
        for place, single in enumerate(singles):
            single[...] = sums[place : place + 1]
        for chip in range(chips):
            both = r.ends[chip] + r.ends[chips + chip]
            r.b_fc[:, chip * units : (chip + 1) * units] = both[6:7, :units]
            here = slice(chip * head_width, (chip + 1) * head_width)
            r.b_qv[0:1, here] = both[7:8, :head_width]
            r.b_qv[1:2, here] = both[7:8, width // 2 : width // 2 + head_width]
        for target, source in ((r.activations, r.acts), (r.in_grads, r.grads)):
            for micro in range(micro_count):
                rows_of = [
                    source[micro * buckets + bucket].astype(F32)[:, None, :]
                    for bucket in range(buckets)
                ]
                target[micro] = jnp.concatenate(rows_of, axis=1).astype(LOW)
        for target in (r.w_qkv, r.w_out, r.w_fc, r.w_proj):
            target[...] = jnp.zeros_like(target)

    def rows_of_sequence(ref):
        return ref[0].reshape(2 * chips * rows, ref.shape[-1])

    nrm, nmlp, ups, brn, act, gpre, mix = (
        rows_of_sequence(ref)
        for ref in (r.all_nrm, r.all_nmlp, r.all_ups, r.all_brn, r.all_act, r.all_gpre, r.all_mix)
    )
    r.w_proj[...] += dot_tn(act, ups)
    r.w_fc[...] += dot_tn(nmlp, gpre)
    r.w_out[...] += dot_tn(mix, brn)
    for which in range(3):
        grad = r.all_dqkv[0, :, which].reshape(2 * chips * rows, head_width)
        r.w_qkv[which] += dot_tn(grad, nrm)


def weights_call(relayed, inputs_shape, head_width, units):
    lines = lax.axis_size("section")
    chips = lax.axis_size("tensor")
    width = inputs_shape[-1]
    half = width // 2
    outputs = dict(
        activations=(inputs_shape, LOW),
        in_grads=(inputs_shape, LOW),
        ln1_gain=((1, width), F32),
        ln1_shift=((1, width), F32),
        w_qkv=((3, head_width, half), F32),
        b_qv=((2, width), F32),
        w_out=((head_width, half), F32),
        b_out=((1, width), F32),
        ln2_gain=((1, width), F32),
        ln2_shift=((1, width), F32),
        w_fc=((half, units), F32),
        b_fc=((1, chips * units), F32),
        w_proj=((units, half), F32),
        b_proj=((1, width), F32),
    )

    def spec(array):
        if len(array.shape) < 5:
            return pl.BlockSpec(array.shape, lambda step: (0,) * len(array.shape))
        return pl.BlockSpec(
            (1,) + array.shape[1:], lambda step: (step,) + (0,) * (len(array.shape) - 1)
        )

    def whole(shape):
        return pl.BlockSpec(shape, lambda step: (0,) * len(shape))

    return pl.pallas_call(
        functools.partial(weights_kernel, tuple(relayed) + tuple(outputs)),
        out_shape=[jax.ShapeDtypeStruct(shape, kind) for shape, kind in outputs.values()],
        grid=(lines,),
        in_specs=[spec(array) for array in relayed.values()],
        out_specs=[whole(shape) for shape, _ in outputs.values()],
        compiler_params=pltpu.CompilerParams(vmem_limit_bytes=60 * 2**20),
        name="weight_gradients",
    )(*relayed.values())


def on_line(
    inputs,
    cotangent,
    lengths,
    chosen,
    ln1_gain,
    ln1_shift,
    w_qkv,
    b_qv,
    w_out,
    b_out,
    ln2_gain,
    ln2_shift,
    w_fc,
    b_fc,
    w_proj,
    b_proj,
):
    head_width, units = w_out.shape[1], w_fc.shape[2]
    singles = dict(
        ln1_gain=ln1_gain,
        ln1_shift=ln1_shift,
        ln2_gain=ln2_gain,
        ln2_shift=ln2_shift,
        b_out=b_out,
        b_proj=b_proj,
        b_fc=b_fc,
        b_qv=b_qv[0],
    )
    weights = dict(
        wq_in=jnp.swapaxes(w_qkv[0], 1, 2).reshape(-1, inputs.shape[-1]),
        wo_in=w_out[0],
        wf_in=w_fc[0],
        wp_in=w_proj[0],
    )
    picks = chosen.reshape((-1,) + chosen.shape[-2:])
    relayed = relay_call(inputs, cotangent, lengths, picks, singles, weights)
    results = list(weights_call(relayed, inputs.shape, head_width, units))
    results[4] = jnp.swapaxes(results[4], 1, 2)
    vectors = (2, 3, 7, 8, 9, 11, 13)
    return tuple(
        result if place in vectors else result[None] for place, result in enumerate(results)
    )


def fits_lines(mesh):
    return mesh.shape["section"] == 4 and mesh.shape["seq"] == 2 and mesh.shape["tensor"] == 4


def solution(mesh):
    placed = (
        P(None, ("seq", "tensor"), None, None),
        P(None, ("seq", "tensor"), None, None),
        P(),
        P("section", None, None, "tensor", "seq", None),
        P("section", None),
        P("section", None),
        P("section", None, None, "tensor"),
        P("section", None, "tensor"),
        P("section", "tensor", None),
        P("section", None),
        P("section", None),
        P("section", None),
        P("section", None, "tensor"),
        P("section", "tensor"),
        P("section", "tensor", None),
        P("section", None),
    )
    return jax.shard_map(
        on_line if fits_lines(mesh) else on_device,
        mesh=mesh,
        in_specs=placed,
        out_specs=(
            P("section", None, ("seq", "tensor"), None, None),
            P("section", None, ("seq", "tensor"), None, None),
            P("section", None),
            P("section", None),
            P("section", None, "seq", "tensor"),
            P("section", None, None),
            P("section", "tensor", "seq"),
            P("section", None),
            P("section", None),
            P("section", None),
            P("section", "seq", "tensor"),
            P("section", None),
            P("section", "tensor", "seq"),
            P("section", None),
        ),
        check_vma=False,
    )
```

```python
import functools
import types

import jax
import jax.numpy as jnp
from jax import lax
from jax.experimental import pallas as pl
from jax.experimental.pallas import tpu as pltpu
from jax.sharding import PartitionSpec as P

HDIM = 64
WIN = 64
QB = 64
KSEL = 64


NORM_EPS = 1e-05
MASKED = -1000000000.0


def from_behind(value, axis, steps):
    count = lax.axis_size(axis)
    first, last = (max(0, -steps), min(count, count - steps))
    return lax.ppermute(value, axis, [(source, source + steps) for source in range(first, last)])


def layer_norm(values, gain, shift):
    average = jnp.mean(values, axis=-1, keepdims=True)
    centred = values - average
    variance = jnp.mean(centred * centred, axis=-1, keepdims=True)
    return centred * lax.rsqrt(variance + NORM_EPS) * gain + shift


def gelu_tanh(values):
    return (
        0.5
        * values
        * (1.0 + jnp.tanh(0.7978845608028654 * (values + 0.044715 * values * values * values)))
    )


def gather_rows(row_block):
    return lax.all_gather(row_block, "tensor", axis=0, tiled=True)


def scatter_product(left_rows, weight, formula):
    return lax.psum_scatter(
        jnp.einsum(formula, left_rows, weight, preferred_element_type=jnp.float32).astype(
            jnp.bfloat16
        ),
        "tensor",
        scatter_dimension=0,
        tiled=True,
    ).astype(jnp.float32)


def near_slabs(full_rows, seq_start, seq_first, length_local):
    buckets = full_rows.shape[1]
    heads_local = full_rows.shape[2] // HDIM
    blocks = length_local // QB
    earlier = lax.dynamic_slice_in_dim(full_rows, jnp.maximum(seq_start - WIN, 0), WIN, 0)
    earlier = jnp.where(seq_first, jnp.zeros_like(earlier), earlier)
    local_part = lax.dynamic_slice_in_dim(full_rows, seq_start, length_local, 0)
    segment = jnp.concatenate([earlier, local_part], 0).reshape(
        length_local + WIN, buckets, heads_local, HDIM
    )
    return jnp.concatenate(
        [
            segment[offset_index * QB : offset_index * QB + length_local].reshape(
                blocks, QB, buckets, heads_local, HDIM
            )
            for offset_index in range(WIN // QB + 1)
        ],
        1,
    )


def far_rows(full_rows, flat_index):
    total_rows, buckets, feature_width = full_rows.shape
    heads_local = feature_width // HDIM
    return jnp.take(full_rows.reshape(total_rows * buckets * heads_local, HDIM), flat_index, axis=0)


def key_geometry(chosen_now, seq_start, blocks):
    buckets, heads_local = (chosen_now.shape[0], chosen_now.shape[1])
    bucket_ids = lax.broadcasted_iota(jnp.int32, chosen_now.shape, 0)
    head_ids = lax.broadcasted_iota(jnp.int32, chosen_now.shape, 1)
    flat_index = (chosen_now * buckets + bucket_ids) * heads_local + head_ids
    block_start = seq_start + QB * lax.broadcasted_iota(jnp.int32, (blocks, 1, 1), 0)
    query_ids = lax.broadcasted_iota(jnp.int32, (1, QB, 1), 1)
    key_ids = lax.broadcasted_iota(jnp.int32, (1, 1, WIN + QB), 2)
    distance = query_ids + WIN - key_ids
    near_ok = (distance >= 0) & (distance < WIN) & (block_start + key_ids - WIN >= 0)
    far_ok = chosen_now + WIN <= block_start.reshape(1, 1, blocks, 1)
    near_mask = jnp.broadcast_to(
        near_ok[:, None, None], (blocks, buckets, heads_local, QB, WIN + QB)
    )
    far_mask = jnp.broadcast_to(
        jnp.transpose(far_ok, (2, 0, 1, 3))[:, :, :, None, :],
        (blocks, buckets, heads_local, QB, KSEL),
    )
    return (flat_index, jnp.concatenate([near_mask, far_mask], -1))


def attention_setup(queries, key_rows, value_rows, chosen_now, seq_start, seq_first):
    length_local, buckets, feature_width = queries.shape
    heads_local = feature_width // HDIM
    blocks = length_local // QB
    query_blocks = queries.reshape(blocks, QB, buckets, heads_local, HDIM)
    flat_index, key_mask = key_geometry(chosen_now, seq_start, blocks)
    near_keys = near_slabs(key_rows, seq_start, seq_first, length_local)
    near_values = near_slabs(value_rows, seq_start, seq_first, length_local)
    far_keys = far_rows(key_rows, flat_index)
    far_values = far_rows(value_rows, flat_index)
    near_scores = jnp.einsum(
        "bqnhe,btnhe->bnhqt", query_blocks, near_keys, preferred_element_type=jnp.float32
    )
    far_scores = jnp.einsum(
        "bqnhe,nhbke->bnhqk", query_blocks, far_keys, preferred_element_type=jnp.float32
    )
    scores = jnp.where(
        key_mask, HDIM ** (-0.5) * jnp.concatenate([near_scores, far_scores], -1), MASKED
    )
    return (query_blocks, near_keys, near_values, far_keys, far_values, flat_index, scores)


def attend(queries, key_rows, value_rows, chosen_now, seq_start, seq_first):
    query_blocks, near_keys, near_values, far_keys, far_values, flat_index, scores = (
        attention_setup(queries, key_rows, value_rows, chosen_now, seq_start, seq_first)
    )
    span = WIN + QB
    row_top = jnp.max(scores, -1, keepdims=True)
    exp_terms = jnp.exp(scores - row_top)
    row_total = jnp.sum(exp_terms, -1, keepdims=True)
    softmax_low = (exp_terms / row_total).astype(jnp.bfloat16)
    near_part = jnp.einsum(
        "bnhqt,btnhe->bqnhe",
        softmax_low[..., :span],
        near_values,
        preferred_element_type=jnp.float32,
    )
    far_part = jnp.einsum(
        "bnhqk,nhbke->bqnhe",
        softmax_low[..., span:],
        far_values,
        preferred_element_type=jnp.float32,
    )
    return ((near_part + far_part).reshape(queries.shape), row_top + jnp.log(row_total))


def spread_back(near_grad, far_grad, flat_index, seq_start, seq_first, total_rows):
    blocks, span, buckets, heads_local, head_size = near_grad.shape
    length_local = blocks * QB
    feature_width = heads_local * head_size
    segment = jnp.zeros((length_local + WIN, buckets, heads_local, head_size), jnp.float32)
    for offset_index in range(WIN // QB + 1):
        piece = near_grad[:, offset_index * QB : (offset_index + 1) * QB].reshape(
            length_local, buckets, heads_local, head_size
        )
        segment = segment.at[offset_index * QB : offset_index * QB + length_local].add(piece)
    full_rows = jnp.zeros((total_rows * buckets * heads_local, head_size), jnp.float32)
    full_rows = full_rows.at[flat_index.reshape(-1)].add(far_grad.reshape(-1, head_size))
    full_rows = full_rows.reshape(total_rows, buckets, feature_width)
    local_part = segment[WIN:].reshape(length_local, buckets, feature_width)
    earlier = jnp.where(seq_first, 0.0, segment[:WIN].reshape(WIN, buckets, feature_width))
    full_rows = lax.dynamic_update_slice_in_dim(
        full_rows,
        lax.dynamic_slice_in_dim(full_rows, seq_start, length_local, 0) + local_part,
        seq_start,
        0,
    )
    earlier_start = jnp.maximum(seq_start - WIN, 0)
    full_rows = lax.dynamic_update_slice_in_dim(
        full_rows,
        lax.dynamic_slice_in_dim(full_rows, earlier_start, WIN, 0) + earlier,
        earlier_start,
        0,
    )
    return full_rows


def attend_back(
    queries, key_rows, value_rows, chosen_now, seq_start, seq_first, log_total, grad_mixed
):
    query_blocks, near_keys, near_values, far_keys, far_values, flat_index, scores = (
        attention_setup(queries, key_rows, value_rows, chosen_now, seq_start, seq_first)
    )
    span = WIN + QB
    score_scale = HDIM ** (-0.5)
    grad_blocks = grad_mixed.reshape(query_blocks.shape)
    weights_full = jnp.exp(scores - log_total)
    softmax_low = weights_full.astype(jnp.bfloat16)
    grad_near_weights = jnp.einsum(
        "bqnhe,btnhe->bnhqt", grad_blocks, near_values, preferred_element_type=jnp.float32
    )
    grad_far_weights = jnp.einsum(
        "bqnhe,nhbke->bnhqk", grad_blocks, far_values, preferred_element_type=jnp.float32
    )
    grad_weights = jnp.concatenate([grad_near_weights, grad_far_weights], -1)
    row_dot = jnp.sum(weights_full * grad_weights, -1, keepdims=True)
    grad_scores = (weights_full * (grad_weights - row_dot)).astype(jnp.bfloat16)
    grad_near, grad_far = (grad_scores[..., :span], grad_scores[..., span:])
    grad_queries = score_scale * (
        jnp.einsum("bnhqt,btnhe->bqnhe", grad_near, near_keys, preferred_element_type=jnp.float32)
        + jnp.einsum("bnhqk,nhbke->bqnhe", grad_far, far_keys, preferred_element_type=jnp.float32)
    )
    near_key_grad = score_scale * jnp.einsum(
        "bnhqt,bqnhe->btnhe", grad_near, query_blocks, preferred_element_type=jnp.float32
    )
    far_key_grad = score_scale * jnp.einsum(
        "bnhqk,bqnhe->nhbke", grad_far, query_blocks, preferred_element_type=jnp.float32
    )
    near_value_grad = jnp.einsum(
        "bnhqt,bqnhe->btnhe",
        softmax_low[..., :span],
        grad_blocks,
        preferred_element_type=jnp.float32,
    )
    far_value_grad = jnp.einsum(
        "bnhqk,bqnhe->nhbke",
        softmax_low[..., span:],
        grad_blocks,
        preferred_element_type=jnp.float32,
    )
    total_rows = key_rows.shape[0]
    key_grad = spread_back(
        near_key_grad, far_key_grad, flat_index, seq_start, seq_first, total_rows
    )
    value_grad = spread_back(
        near_value_grad, far_value_grad, flat_index, seq_start, seq_first, total_rows
    )
    return (grad_queries.reshape(queries.shape), key_grad, value_grad)


def forward_pass(hidden, params, chosen_now, query_mask, seq_start, seq_first, finish):
    (
        ln1_gain,
        ln1_shift,
        w_qkv,
        b_qv,
        w_out,
        b_out,
        ln2_gain,
        ln2_shift,
        w_fc,
        b_fc,
        w_proj,
        b_proj,
    ) = params
    hidden_wide = hidden.astype(jnp.float32)
    normed_all = gather_rows(layer_norm(hidden_wide, ln1_gain, ln1_shift).astype(jnp.bfloat16))
    projected = jnp.einsum("pnd,jdc->jpnc", normed_all, w_qkv, preferred_element_type=jnp.float32)
    queries = (projected[0] + b_qv[0]).astype(jnp.bfloat16)
    key_rows, value_rows = (
        lax.all_gather(projected[1].astype(jnp.bfloat16), "seq", axis=0, tiled=True),
        lax.all_gather((projected[2] + b_qv[1]).astype(jnp.bfloat16), "seq", axis=0, tiled=True),
    )
    attended, log_total = attend(queries, key_rows, value_rows, chosen_now, seq_start, seq_first)
    mixed_rows = (attended * query_mask[:, :, None]).astype(jnp.bfloat16)
    middle = hidden_wide + scatter_product(mixed_rows, w_out, "pnc,cd->pnd") + b_out
    normed_mlp = gather_rows(layer_norm(middle, ln2_gain, ln2_shift).astype(jnp.bfloat16))
    pre_active = (
        jnp.einsum("pnd,df->pnf", normed_mlp, w_fc, preferred_element_type=jnp.float32) + b_fc
    )
    active = gelu_tanh(pre_active).astype(jnp.bfloat16)
    if not finish:
        return (
            normed_all,
            queries,
            key_rows,
            value_rows,
            log_total,
            mixed_rows,
            middle,
            normed_mlp,
            pre_active,
            active,
        )
    output = (middle + scatter_product(active, w_proj, "pnf,fd->pnd") + b_proj).astype(jnp.bfloat16)
    return (output, (key_rows, value_rows))


def backward_pass(hidden, upstream, params, chosen_now, query_mask, seq_start, seq_first):
    (
        ln1_gain,
        ln1_shift,
        w_qkv,
        b_qv,
        w_out,
        b_out,
        ln2_gain,
        ln2_shift,
        w_fc,
        b_fc,
        w_proj,
        b_proj,
    ) = params
    (
        normed_all,
        queries,
        key_rows,
        value_rows,
        log_total,
        mixed_rows,
        middle,
        normed_mlp,
        pre_active,
        active,
    ) = forward_pass(hidden, params, chosen_now, query_mask, seq_start, seq_first, False)
    upstream_all = gather_rows(upstream)
    grad_w_proj = jnp.einsum(
        "pnf,pnd->fd", active, upstream_all, preferred_element_type=jnp.float32
    )
    grad_b_proj = jnp.sum(upstream.astype(jnp.float32), axis=(0, 1))
    grad_active = jnp.einsum(
        "pnd,fd->pnf", upstream_all, w_proj, preferred_element_type=jnp.float32
    )
    unused_value, gelu_pull = jax.vjp(gelu_tanh, pre_active)
    grad_pre = gelu_pull(grad_active)[0].astype(jnp.bfloat16)
    grad_w_fc = jnp.einsum("pnd,pnf->df", normed_mlp, grad_pre, preferred_element_type=jnp.float32)
    grad_b_fc = jnp.sum(grad_pre.astype(jnp.float32), axis=(0, 1))
    grad_normed_mlp = scatter_product(grad_pre, w_fc, "pnf,df->pnd")
    unused_norm, second_pull = jax.vjp(layer_norm, middle, ln2_gain, ln2_shift)
    grad_mid_norm, grad_ln2_gain, grad_ln2_shift = second_pull(grad_normed_mlp)
    grad_middle = upstream.astype(jnp.float32) + grad_mid_norm
    grad_branch = grad_middle.astype(jnp.bfloat16)
    grad_b_out = jnp.sum(grad_branch.astype(jnp.float32), axis=(0, 1))
    branch_all = gather_rows(grad_branch)
    grad_w_out = jnp.einsum(
        "pnc,pnd->cd", mixed_rows, branch_all, preferred_element_type=jnp.float32
    )
    grad_mixed = jnp.einsum(
        "pnd,cd->pnc", branch_all, w_out, preferred_element_type=jnp.float32
    ).astype(jnp.bfloat16) * query_mask[:, :, None].astype(jnp.bfloat16)
    grad_queries, key_grad_all, value_grad_all = attend_back(
        queries, key_rows, value_rows, chosen_now, seq_start, seq_first, log_total, grad_mixed
    )
    key_grad, value_grad = (
        lax.psum_scatter(
            key_grad_all.astype(jnp.bfloat16), "seq", scatter_dimension=0, tiled=True
        ).astype(jnp.float32),
        lax.psum_scatter(
            value_grad_all.astype(jnp.bfloat16), "seq", scatter_dimension=0, tiled=True
        ).astype(jnp.float32),
    )
    grad_project = jnp.stack(
        [
            grad_queries.astype(jnp.bfloat16),
            key_grad.astype(jnp.bfloat16),
            value_grad.astype(jnp.bfloat16),
        ],
        2,
    )
    grad_w_qkv = jnp.einsum(
        "pnd,pnjc->jdc", normed_all, grad_project, preferred_element_type=jnp.float32
    )
    grad_b_qv = jnp.sum(grad_project[:, :, 0::2].astype(jnp.float32), axis=(0, 1))
    grad_normed = scatter_product(grad_project, w_qkv, "pnjc,jdc->pnd")
    unused_first, first_pull = jax.vjp(layer_norm, hidden.astype(jnp.float32), ln1_gain, ln1_shift)
    grad_in_norm, grad_ln1_gain, grad_ln1_shift = first_pull(grad_normed)
    grad_hidden = (grad_middle + grad_in_norm).astype(jnp.bfloat16)
    block_grads = (
        grad_ln1_gain,
        grad_ln1_shift,
        grad_w_qkv,
        grad_b_qv,
        grad_w_out,
        grad_b_out,
        grad_ln2_gain,
        grad_ln2_shift,
        grad_w_fc,
        grad_b_fc,
        grad_w_proj,
        grad_b_proj,
    )
    return (grad_hidden, block_grads)


def on_device(
    inputs,
    cotangent,
    lengths,
    chosen,
    ln1_gain,
    ln1_shift,
    w_qkv,
    b_qv,
    w_out,
    b_out,
    ln2_gain,
    ln2_shift,
    w_fc,
    b_fc,
    w_proj,
    b_proj,
):
    params = tuple(
        (
            weight_array[0]
            for weight_array in (
                ln1_gain,
                ln1_shift,
                w_qkv,
                b_qv,
                w_out,
                b_out,
                ln2_gain,
                ln2_shift,
                w_fc,
                b_fc,
                w_proj,
                b_proj,
            )
        )
    )
    section_index = lax.axis_index("section")
    section_count = lax.axis_size("section")
    seq_index = lax.axis_index("seq")
    tensor_index = lax.axis_index("tensor")
    tensor_count = lax.axis_size("tensor")
    micro_count, rows_local, buckets, feature_width = inputs.shape
    length_local = rows_local * tensor_count
    heads_width = w_qkv.shape[-1]
    seq_start = seq_index * length_local
    seq_first = seq_index == 0
    positions = seq_start + lax.broadcasted_iota(jnp.int32, (micro_count, length_local, buckets), 1)
    mask_all = (positions < lengths[:, None, :]).astype(jnp.float32)
    mask_rows = lax.dynamic_slice_in_dim(mask_all, tensor_index * rows_local, rows_local, 1)
    step_count = micro_count + section_count - 1
    chosen_section = chosen[0]
    received = jnp.zeros((rows_local, buckets, feature_width), jnp.bfloat16)
    stored = jnp.zeros((micro_count, rows_local, buckets, feature_width), jnp.bfloat16)
    outputs = jnp.zeros_like(stored)
    for step_index in range(step_count):
        micro_index = step_index - section_index
        running = (micro_index >= 0) & (micro_index < micro_count)
        slot_index = jnp.clip(micro_index, 0, micro_count - 1)
        block_in = jnp.where(
            section_index == 0, lax.dynamic_index_in_dim(inputs, slot_index, 0, False), received
        )
        chosen_now = lax.dynamic_index_in_dim(chosen_section, slot_index, 0, False)
        query_mask = lax.dynamic_index_in_dim(mask_all, slot_index, 0, False)
        result, key_pair = forward_pass(
            block_in, params, chosen_now, query_mask, seq_start, seq_first, True
        )
        stored = jnp.where(
            running, lax.dynamic_update_index_in_dim(stored, block_in, slot_index, 0), stored
        )
        outputs = jnp.where(
            running, lax.dynamic_update_index_in_dim(outputs, result, slot_index, 0), outputs
        )
        received = from_behind(result, "section", 1)
    back_received = jnp.zeros((rows_local, buckets, feature_width), jnp.bfloat16)
    in_grads = jnp.zeros_like(stored)
    totals = None
    for step_index in range(step_count):
        micro_index = step_index - (section_count - 1 - section_index)
        running = (micro_index >= 0) & (micro_index < micro_count)
        slot_index = jnp.clip(micro_index, 0, micro_count - 1)
        chosen_now = lax.dynamic_index_in_dim(chosen_section, slot_index, 0, False)
        query_mask = lax.dynamic_index_in_dim(mask_all, slot_index, 0, False)
        local_mask = lax.dynamic_index_in_dim(mask_rows, slot_index, 0, False)
        top_grad = (
            lax.dynamic_index_in_dim(cotangent, slot_index, 0, False).astype(jnp.float32)
            * local_mask[:, :, None]
        ).astype(jnp.bfloat16)
        upstream = jnp.where(section_index == section_count - 1, top_grad, back_received)
        hidden = lax.dynamic_index_in_dim(stored, slot_index, 0, False)
        grad_hidden, block_grads = backward_pass(
            hidden, upstream, params, chosen_now, query_mask, seq_start, seq_first
        )
        block_grads = tuple(
            (jnp.where(running, grad_part, jnp.zeros_like(grad_part)) for grad_part in block_grads)
        )
        totals = (
            block_grads
            if step_index == 0
            else tuple(
                (total_part + grad_part for total_part, grad_part in zip(totals, block_grads))
            )
        )
        in_grads = jnp.where(
            running, lax.dynamic_update_index_in_dim(in_grads, grad_hidden, slot_index, 0), in_grads
        )
        back_received = from_behind(grad_hidden, "section", -1)
    (
        sum_ln1_gain,
        sum_ln1_shift,
        sum_w_qkv,
        sum_b_qv,
        sum_w_out,
        sum_b_out,
        sum_ln2_gain,
        sum_ln2_shift,
        sum_w_fc,
        sum_b_fc,
        sum_w_proj,
        sum_b_proj,
    ) = totals
    part_qkv, part_out, part_fc, part_proj = (
        lax.psum_scatter(
            sum_w_qkv.astype(jnp.bfloat16), "seq", scatter_dimension=1, tiled=True
        ).astype(jnp.float32),
        lax.psum_scatter(
            sum_w_out.astype(jnp.bfloat16), "seq", scatter_dimension=1, tiled=True
        ).astype(jnp.float32),
        lax.psum_scatter(
            sum_w_fc.astype(jnp.bfloat16), "seq", scatter_dimension=0, tiled=True
        ).astype(jnp.float32),
        lax.psum_scatter(
            sum_w_proj.astype(jnp.bfloat16), "seq", scatter_dimension=1, tiled=True
        ).astype(jnp.float32),
    )
    bias_qv = lax.dynamic_update_slice_in_dim(
        jnp.zeros((2, feature_width), jnp.float32), sum_b_qv, tensor_index * heads_width, 1
    )
    units_local = sum_b_fc.shape[0]
    bias_fc = lax.dynamic_update_slice_in_dim(
        jnp.zeros((units_local * tensor_count,), jnp.float32),
        sum_b_fc,
        tensor_index * units_local,
        0,
    )
    small_sums = lax.psum(
        (
            sum_ln1_gain,
            sum_ln1_shift,
            bias_qv,
            sum_b_out,
            sum_ln2_gain,
            sum_ln2_shift,
            bias_fc,
            sum_b_proj,
        ),
        ("seq", "tensor"),
    )
    return (
        outputs[None],
        in_grads[None],
        small_sums[0][None],
        small_sums[1][None],
        part_qkv[None],
        small_sums[2][None],
        part_out[None],
        small_sums[3][None],
        small_sums[4][None],
        small_sums[5][None],
        part_fc[None],
        small_sums[6][None],
        part_proj[None],
        small_sums[7][None],
    )


STREAMS = 2
NRM, NMLP, UPS, BRN, ACT, GPRE, MIX, DQKV = range(8)
F32 = jnp.float32
LOW = jnp.bfloat16
MESH_ID = pl.DeviceIdType.MESH


def dot_nn(left, right):
    return lax.dot_general(left, right, (((1,), (0,)), ((), ())), preferred_element_type=F32)


def dot_nt(left, right):
    return lax.dot_general(left, right, (((1,), (1,)), ((), ())), preferred_element_type=F32)


def dot_tn(left, right):
    return lax.dot_general(left, right, (((0,), (0,)), ((), ())), preferred_element_type=F32)


def standard(rows):
    centred = rows - jnp.mean(rows, axis=-1, keepdims=True)
    scale = lax.rsqrt(jnp.mean(centred * centred, axis=-1, keepdims=True) + NORM_EPS)
    return centred * scale, scale


def standard_back(grad, xhat, scale):
    inner = jnp.mean(grad * xhat, axis=-1, keepdims=True)
    return scale * (grad - jnp.mean(grad, axis=-1, keepdims=True) - xhat * inner)


def column_sum(rows):
    return jnp.sum(rows.astype(F32), axis=0, keepdims=True)


def relay_kernel(names, *refs):
    r = types.SimpleNamespace(**dict(zip(names, refs)))
    a, c, t = (lax.axis_index(name) for name in ("section", "seq", "tensor"))
    lines = lax.axis_size("section")
    chips = lax.axis_size("tensor")
    rows, buckets, width = r.inputs.shape[1:]
    half_width = width // 2
    local = rows * chips
    total = 2 * local
    stream_rows = local // STREAMS
    head_width = r.wo_in.shape[0]
    heads = head_width // HDIM
    blocks = local // QB
    units = r.wp_in.shape[0]
    scale = HDIM ** (-0.5)
    streams = range(STREAMS)

    def remote(src, dst, send, recv, **target):
        return pltpu.make_async_remote_copy(
            src_ref=src,
            dst_ref=dst,
            send_sem=send,
            recv_sem=recv,
            device_id=target,
            device_id_type=MESH_ID,
        )

    def drain(ref, sem):
        pltpu.make_async_copy(ref, ref, sem).wait()

    def row_block(index, size):
        return pl.ds(pl.multiple_of(index * size, size), size)

    near_chip = t + 1 - 2 * (t % 2)
    over_chip = (t + 2) % 4
    across_chip = 3 - t
    middle_chip = (t == 1) | (t == 2)
    end_chip = (t == 0) | (t == 3)
    owned = stream_rows // 2
    mine = row_block(t - 1, owned)
    my_half = row_block(c, local)

    barrier = pltpu.get_barrier_semaphore()
    for core in range(2):
        for step in range(1, chips):
            there = {"tensor": (t + step) % chips, "seq": core}
            pl.semaphore_signal(barrier, inc=1, device_id=there, device_id_type=MESH_ID)
        for step in range(1, lines):
            there = {"section": (a + step) % lines, "seq": core}
            pl.semaphore_signal(barrier, inc=1, device_id=there, device_id_type=MESH_ID)
    for step in range(1, lines):
        there = {"section": (a + step) % lines, "tensor": near_chip}
        pl.semaphore_signal(barrier, inc=1, device_id=there, device_id_type=MESH_ID)
    pl.semaphore_signal(barrier, inc=1, device_id={"seq": 1 - c}, device_id_type=MESH_ID)
    pl.semaphore_wait(barrier, 2 * (chips - 1) + 3 * (lines - 1) + 1)

    def beside(s):
        return s + 1 - 2 * (s % 2)

    def above(s):
        return (s + 2) % 4

    def store(p):
        return (r.wq, r.wo, r.wf, r.wp)[p]

    def source(p):
        return (r.wq_in, r.wo_in, r.wf_in, r.wp_in)[p]

    def height(p):
        return source(p).shape[0]

    def core_half(p, s, core):
        return store(p).at[s, row_block(core, height(p) // 2)]

    def first_hop(p, s, neighbour, which):
        return remote(
            source(p).at[row_block(c, height(p) // 2)],
            core_half(p, s, c),
            r.w_first_s.at[p, which],
            r.w_first_r.at[s, p],
            section=neighbour,
        )

    def second_hop(p, s, which):
        view = store(p).at[s, row_block(2 * c + which, height(p) // 4)]
        return remote(
            view, view, r.w_second_s.at[s, p], r.w_second_r.at[s, p, which], section=3 - s
        )

    def core_hop(p, s, core):
        view = core_half(p, s, core)
        return remote(view, view, r.w_core_s.at[s, p], r.w_core_r.at[s, p], seq=1 - c)

    def own_copy(p):
        return pltpu.make_async_copy(source(p), store(p).at[a], r.w_own.at[p])

    def pass_on(s, p, which):
        line = (beside(s), above(s))[which]

        @pl.when(a == line)
        def _():
            first_hop(p, s, line, which).wait_recv()
            second_hop(p, s, which).start()
            core_hop(p, s, c).start()

    def pass_all(s, pieces):
        for p in pieces:
            for which in range(2):
                pass_on(s, p, which)

    def pass_far(s, p):
        @pl.when(a == 3 - s)
        def _():
            second_hop(p, s, 0).wait_recv()
            second_hop(p, s, 1).wait_recv()
            core_hop(p, s, c).start()

    def need(s, p):
        @pl.when(s == 0)
        def _():
            if p < 2:
                pass_all(0, (p,))
            pass_far(0, p)

        @pl.when(a == s)
        def _():
            own_copy(p).wait()

        @pl.when(a != s)
        def _():
            core_hop(p, s, 1 - c).wait_recv()

    def small_copy(step, line, slot):
        return remote(
            r.small_own, r.small.at[slot], r.small_s.at[step], r.small_r.at[slot], section=line
        )

    def count_copy(step, line, slot):
        return remote(
            r.count_own.at[line],
            r.count.at[slot],
            r.count_s.at[step],
            r.count_r.at[slot],
            section=line,
        )

    singles = (r.ln1_gain, r.ln1_shift, r.ln2_gain, r.ln2_shift, r.b_out, r.b_proj)
    for place, single in enumerate(singles):
        r.small_own[place : place + 1] = single[...]
    r.small_own[6:7, :units] = r.b_fc[...]
    r.small_own[7:8, :head_width] = r.b_qv[0:1]
    r.small_own[7:8, half_width : half_width + head_width] = r.b_qv[1:2]
    for step in range(1, lines):
        small_copy(step - 1, (a + step) % lines, a).start()
    for p in range(4):
        for which, line in enumerate((beside(a), above(a))):
            first_hop(p, a, line, which).start()
    for p in range(4):
        own_copy(p).start()
    r.small[a] = r.small_own[...]

    def place_of(index):
        inside = index % local
        stream, left = inside // stream_rows, inside % stream_rows
        first = (index // local) * local + (left // owned) * (local // 2)
        return first + stream * owned + left % owned

    def iota(shape, dimension):
        return lax.broadcasted_iota(jnp.int32, shape, dimension)

    square = jnp.where(iota((KSEL, KSEL), 0) == iota((KSEL, KSEL), 1), 1.0, 0.0).astype(LOW)
    position = place_of(iota((KSEL, total), 1)).astype(F32)
    for pair in range(lines * heads):
        line, head = pair // heads, pair % heads
        columns = dot_nt(square, r.chosen[pair].astype(F32).astype(LOW))
        for block in range(blocks):
            pick = head * blocks + block
            r.count_own[line, pick : pick + 1, :] = jnp.sum(
                jnp.where(columns[:, block : block + 1] == position, 1.0, 0.0),
                axis=0,
                keepdims=True,
            )
    for step in range(1, lines):
        count_copy(step - 1, (a + step) % lines, a).start()
    r.count[a] = r.count_own[a]

    NEAR, OVER, ACROSS = range(3)

    def gather(buffer, s, kind, j, owner, target, slot):
        view = buffer.at[s, j, row_block(owner - 1, owned)]
        return remote(
            view, view, r.ag_s.at[kind, j, slot], r.ag_r.at[kind, j, slot], tensor=target
        )

    def used_before(s, kind):
        return s > 0 if kind < 2 else s < lines - 1

    def gather_start(buffer, s, kind, j):
        @pl.when(used_before(s, kind))
        def _():
            gather_sent(buffer, s, kind, j)

        gather(buffer, s, kind, j, t, over_chip, OVER).start()
        gather(buffer, s, kind, j, t, across_chip, ACROSS).start()
        gather(buffer, s, kind, j, t, near_chip, NEAR).start()

    def gather_wait(buffer, s, kind, j):
        @pl.when(middle_chip)
        def _():
            gather(buffer, s, kind, j, across_chip, across_chip, ACROSS).wait_recv()

        @pl.when(end_chip)
        def _():
            gather(buffer, s, kind, j, near_chip, near_chip, NEAR).wait_recv()
            gather(buffer, s, kind, j, over_chip, over_chip, OVER).wait_recv()

    def gather_sent(buffer, s, kind, j):
        gather(buffer, s, kind, j, t, over_chip, OVER).wait_send()
        gather(buffer, s, kind, j, t, across_chip, ACROSS).wait_send()
        gather(buffer, s, kind, j, t, near_chip, NEAR).wait_send()

    def scatter(s, kind, j, owner, slot):
        return remote(
            r.part.at[kind, j, row_block(owner - 1, owned)],
            r.arrived.at[s, kind, j, slot],
            r.rs_s.at[kind, j, slot],
            r.rs_r.at[kind, j, slot],
            tensor=owner,
        )

    def scatter_start(s, kind, j, product):
        @pl.when(used_before(s, kind))
        def _():
            scatter_sent(s, kind, j)

        r.part[kind, j] = product.astype(LOW)
        scatter_send(s, kind, j)

    def scatter_all(s, kind, product):
        r.part[kind] = product.astype(LOW).reshape(r.part.shape[1:])
        for j in streams:
            scatter_send(s, kind, j)

    def scatter_free(s, kind):
        @pl.when(used_before(s, kind))
        def _():
            for j in streams:
                scatter_sent(s, kind, j)

    def scatter_send(s, kind, j):
        @pl.when(end_chip)
        def _():
            scatter(s, kind, j, over_chip, OVER).start()
            scatter(s, kind, j, near_chip, NEAR).start()

        @pl.when(middle_chip)
        def _():
            scatter(s, kind, j, across_chip, ACROSS).start()

    def scatter_sum(s, kind, j):
        result = r.part[kind, j, mine].astype(F32)
        for slot in (NEAR, ACROSS, OVER):
            scatter(s, kind, j, t, slot).wait_recv()
            result = result + r.arrived[s, kind, j, slot].astype(F32)
        return result

    def scatter_sent(s, kind, j):
        @pl.when(end_chip)
        def _():
            scatter(s, kind, j, over_chip, OVER).wait_send()
            scatter(s, kind, j, near_chip, NEAR).wait_send()

        @pl.when(middle_chip)
        def _():
            scatter(s, kind, j, across_chip, ACROSS).wait_send()

    own_rows = (r.nrm, r.nmlp, r.ups, r.brn, r.act, r.gpre, r.mix, r.dqkv)
    all_rows = (
        r.all_nrm,
        r.all_nmlp,
        r.all_ups,
        r.all_brn,
        r.all_act,
        r.all_gpre,
        r.all_mix,
        r.all_dqkv,
    )

    def rows_copy(index, s, same, stays=False):
        core = c if same else 1 - c
        src = own_rows[index].at[s]
        dst = all_rows[index].at[a, c]
        if index <= BRN:
            src = src.at[:, :, row_block(core, half_width)]
        recv = r.rows_r.at[index]
        if stays:
            return pltpu.make_async_copy(src, dst, recv)
        if same:
            return remote(src, dst, r.rows_s.at[index, s, 0], recv, section=s)
        return remote(src, dst, r.rows_s.at[index, s, 1], recv, section=s, seq=1 - c)

    def rows_start(index, s):
        @pl.when(a == s)
        def _():
            rows_copy(index, s, True, True).start()

        @pl.when(a != s)
        def _():
            rows_copy(index, s, True).start()

        if index <= BRN:
            rows_copy(index, s, False).start()

    def forward_rows(s):
        for index in (NRM, MIX, NMLP, ACT):
            rows_start(index, s)

    def rows_sent(index, s):
        @pl.when(a != s)
        def _():
            rows_copy(index, s, True).wait_send()

        if index <= BRN:
            rows_copy(index, s, False).wait_send()

    def share_copy(index, core):
        view = all_rows[index].at[:, core]
        return remote(view, view, r.share_s.at[index - ACT], r.share_r.at[index - ACT], seq=1 - c)

    def share(index):
        drain(all_rows[index].at[:, c], r.rows_r.at[index])
        share_copy(index, c).start()

    def norm_copy(s):
        return remote(
            r.norm_part.at[s], r.norm_all.at[a], r.norm_s.at[s], r.norm_r, section=s
        )

    def norm_start(s):
        @pl.when(a == s)
        def _():
            pltpu.make_async_copy(r.norm_part.at[s], r.norm_all.at[a], r.norm_r).start()

        @pl.when(a != s)
        def _():
            norm_copy(s).start()

    def home_copy(what, s, chip):
        src, dst, send, recv = what
        return remote(
            src.at[s, chip % 2],
            dst.at[a],
            send.at[s, chip % 2],
            recv,
            section=s,
            tensor=chip,
        )

    def home_start(what, s):
        src, dst, send, recv = what

        @pl.when(middle_chip & (a == s))
        def _():
            pltpu.make_async_copy(src.at[s, t % 2], dst.at[a], recv).start()

        @pl.when(middle_chip & (a != s))
        def _():
            home_copy(what, s, t).start()

        @pl.when(middle_chip)
        def _():
            home_copy(what, s, near_chip).start()

    def home_sent(what, s):
        @pl.when(middle_chip & (a != s))
        def _():
            home_copy(what, s, t).wait_send()

        @pl.when(middle_chip)
        def _():
            home_copy(what, s, near_chip).wait_send()

    out_home = (r.out_low, r.acts, r.out_s, r.out_r)
    grad_home = (r.grad_low, r.grads, r.grad_s, r.grad_r)

    length = r.lengths[a // buckets, a % buckets]
    key = place_of(iota((stream_rows, total), 1))
    for j in streams:
        query = place_of(c * local + j * stream_rows + iota((stream_rows, total), 0))
        r.near[j] = jnp.where((query >= key) & (query - key < WIN), 1.0, 0.0)
    key_row = place_of(iota((1, total), 1))

    def row_mask(place):
        return jnp.where(place < length, 1.0, 0.0)

    def multiplicity(s, head):
        far = []
        for block in range(blocks):
            pick = head * blocks + block
            limit = (c * blocks + block) * QB - WIN
            counted = jnp.where(key_row <= limit, r.count[s, pick : pick + 1, :], 0.0)
            far.append(jnp.broadcast_to(counted, (stream_rows // blocks, total)))
        return flat(r.near) + jnp.concatenate(far * STREAMS, axis=0)

    def flat(ref):
        return ref[...].reshape(local, ref.shape[-1])

    def head_cols(head):
        return slice(head * HDIM, (head + 1) * HDIM)

    def kv_copy(s):
        view = r.kv.at[s, :, 0:local]
        return remote(view, view, r.kv_s.at[s], r.kv_r.at[s], seq=1 - c)

    def dkv_copy(s):
        return remote(r.dkv_out.at[s], r.dkv_in.at[s], r.dkv_s.at[s], r.dkv_r.at[s], seq=1 - c)

    def own_sequence(ref):
        both = ref[a // buckets].astype(F32)
        picked = both[:, 0, :]
        for bucket in range(1, buckets):
            picked = jnp.where(a % buckets == bucket, both[:, bucket, :], picked)
        return picked

    def own_part(j):
        chip, first = (j * owned) // rows, (j * owned) % rows
        return chip, slice(first, first + owned)

    def first_copy():
        return remote(r.first_out, r.first_in, r.first_s, r.first_r, tensor=near_chip)

    own_place = c * local + t * rows + iota((rows, 1), 0)
    r.first_out[0] = own_sequence(r.inputs).astype(LOW)
    r.first_out[1] = (own_sequence(r.cotangent) * row_mask(own_place)).astype(LOW)
    r.norm_part[...] = jnp.zeros_like(r.norm_part)

    @pl.when(c == 0)
    def _():
        r.kv[:, :, local:total] = jnp.zeros((lines, 2, local, head_width), LOW)


    @pl.when(end_chip)
    def _():
        first_copy().start()

    @pl.when(middle_chip)
    def _():
        first_copy().wait_recv()
        for which in range(2):
            here, beside_it = r.first_out[which].astype(F32), r.first_in[which].astype(F32)
            lower = jnp.where(t % 2 == 0, here, beside_it)
            upper = jnp.where(t % 2 == 0, beside_it, here)
            for j in streams:
                chip, part = own_part(j)
                own_block = (lower, upper)[chip][part]
                if which == 0:
                    r.hidden[j] = own_block
                else:
                    r.upstream[j] = own_block.astype(LOW)

    def on_owner(stage):
        def run(s, j):
            @pl.when(middle_chip)
            def _():
                stage(s, j)

        return run

    def keep_rows(target, s, j, result):
        chip, part = own_part(j)
        target[s, chip, part] = result

    @on_owner
    def enter(s, j):
        xhat, inverse = standard(r.hidden[j])
        r.xhat1[s, j] = xhat
        r.inv1[s, j] = jnp.broadcast_to(inverse, (owned, 128))
        r.nrm[s, j, mine] = (xhat * r.small[s, 0:1] + r.small[s, 1:2]).astype(LOW)
        gather_start(r.nrm, s, 0, j)

    def project(s, j):
        gather_wait(r.nrm, s, 0, j)
        normed = r.nrm[s, j]
        place = row_block(c * STREAMS + j, stream_rows)
        bias_v = r.small[s, 7:8, half_width : half_width + head_width]
        key_rows = dot_nt(normed, r.wq[s, head_width : 2 * head_width])
        value_rows = dot_nt(normed, r.wq[s, 2 * head_width : 3 * head_width]) + bias_v
        r.kv[s, 0, place] = key_rows.astype(LOW)
        r.kv[s, 1, place] = value_rows.astype(LOW)

    def ask(s, j):
        queries = dot_nt(r.nrm[s, j], r.wq[s, 0:head_width]) + r.small[s, 7:8, :head_width]
        r.qry[s, j] = queries.astype(LOW)

    def attend_line(s):
        mixed = []
        queries = flat(r.qry.at[s])
        for head in range(heads):
            cols = head_cols(head)
            times = multiplicity(s, head)
            scores = scale * dot_nt(queries[:, cols], r.kv[s, 0, :, cols])
            scores = jnp.where(times > 0.0, scores, MASKED)
            top = jnp.max(scores, axis=-1, keepdims=True)
            terms = times * jnp.exp(scores - top)
            weights = terms / jnp.sum(terms, axis=-1, keepdims=True)
            r.soft[s, head] = weights
            mixed.append(dot_nn(weights.astype(LOW), r.kv[s, 1, :, cols]))
        mask = row_mask(place_of(c * local + iota((local, 1), 0)))
        mixed = (jnp.concatenate(mixed, axis=-1) * mask).astype(LOW)
        r.mix[s] = mixed.reshape(r.mix.shape[1:])
        scatter_all(s, 0, dot_nn(mixed, r.wo[s]))

    @on_owner
    def between(s, j):
        middle = r.hidden[j] + scatter_sum(s, 0, j) + r.small[s, 4:5]
        r.middle[j] = middle
        xhat, inverse = standard(middle)
        r.xhat2[s, j] = xhat
        r.inv2[s, j] = jnp.broadcast_to(inverse, (owned, 128))
        r.nmlp[s, j, mine] = (xhat * r.small[s, 2:3] + r.small[s, 3:4]).astype(LOW)
        gather_start(r.nmlp, s, 1, j)

    def feed(s, j):
        gather_wait(r.nmlp, s, 1, j)
        before = dot_nn(r.nmlp[s, j], r.wf[s]) + r.small[s, 6:7, :units]
        bend = jnp.tanh(0.7978845608028654 * (before + 0.044715 * before * before * before))
        r.act[s, j] = (0.5 * before * (1.0 + bend)).astype(LOW)
        r.slope[s, j] = 0.5 * (1.0 + bend) + 0.5 * before * (1.0 - bend * bend) * (
            0.7978845608028654 * (1.0 + 3 * 0.044715 * before * before)
        )


    def leave_feed(s, j):
        scatter_start(s, 1, j, dot_nn(r.act[s, j], r.wp[s]))

    @on_owner
    def finish(s, j):
        result = r.middle[j] + scatter_sum(s, 1, j) + r.small[s, 5:6]
        keep_rows(r.out_low, s, j, result.astype(LOW))
        r.hidden[j] = result.astype(LOW).astype(F32)

    def small_ready(s):
        @pl.when(a != s)
        def _():
            small_copy(0, a, s).wait_recv()

    small_ready(0)
    for j in streams:
        enter(0, j)

    def forward(s, _):
        need(s, 0)
        for j in streams:
            project(s, j)

        @pl.when(c == 0)
        def _():
            kv_copy(s).start()

        for j in streams:
            ask(s, j)

        @pl.when(a != s)
        def _():
            count_copy(0, a, s).wait_recv()

        @pl.when(c == 1)
        def _():
            kv_copy(s).wait_recv()

        need(s, 1)
        scatter_free(s, 0)
        attend_line(s)

        @pl.when(s == 0)
        def _():
            pass_all(0, (2,))
            for later in range(1, lines):
                pass_all(later, (0, 1, 2))

        @pl.when(s == 1)
        def _():
            pass_far(1, 2)
            pass_far(1, 3)
            for later in range(2, lines):
                for p in range(4):
                    pass_far(later, p)

        for j in streams:
            between(s, j)
        @pl.when(s == 0)
        def _():
            for later in range(lines):
                pass_all(later, (3,))

        need(s, 2)
        for j in streams:
            feed(s, j)
            if j == 0:
                need(s, 3)
            leave_feed(s, j)


        @pl.when(s >= 2)
        def _():
            forward_rows(s - 2)


        @pl.when(s + 1 < lines)
        def _():
            small_ready(s + 1)

        for j in streams:
            finish(s, j)

            @pl.when(s + 1 < lines)
            def _():
                enter(s + 1, j)

        home_start(out_home, s)

        @pl.when(s == 0)
        def _():
            pass_far(1, 0)
            pass_far(1, 1)

        return 0

    lax.fori_loop(0, lines, forward, 0)

    @on_owner
    def turn(s, j):
        upstream = r.upstream[j]
        r.ups[s, j, mine] = upstream
        gather_start(r.ups, s, 2, j)
        r.norm_part[s, 5:6] += column_sum(upstream)

    def feed_back(s, j):
        gather_wait(r.ups, s, 2, j)
        grad_pre = (dot_nt(r.ups[s, j], r.wp[s]) * r.slope[s, j]).astype(LOW)
        r.gpre[s, j] = grad_pre
        scatter_start(s, 2, j, dot_nt(grad_pre, r.wf[s]))
        r.norm_part[s, 6:7, :units] += column_sum(grad_pre)

    @on_owner
    def between_back(s, j):
        grad = scatter_sum(s, 2, j)
        xhat = r.xhat2[s, j]
        upstream = r.upstream[j].astype(F32)
        grad_middle = upstream + standard_back(
            grad * r.small[s, 2:3], xhat, r.inv2[s, j, :, 0:1]
        )
        r.middle[j] = grad_middle
        branch = grad_middle.astype(LOW)
        r.brn[s, j, mine] = branch
        gather_start(r.brn, s, 3, j)
        r.norm_part[s, 2:3] += column_sum(grad * xhat)
        r.norm_part[s, 3:4] += column_sum(grad)
        r.norm_part[s, 4:5] += column_sum(branch)

    def mixed_back(s, j):
        gather_wait(r.brn, s, 3, j)
        place = place_of(c * local + j * stream_rows + iota((stream_rows, 1), 0))
        r.gmix[j] = (dot_nt(r.brn[s, j], r.wo[s]) * row_mask(place)).astype(LOW)

    def attend_line_back(s):
        grad_q, grad_k, grad_v = [], [], []
        grad_mixed, queries = flat(r.gmix), flat(r.qry.at[s])
        for head in range(heads):
            cols = head_cols(head)
            weights = r.soft[s, head]
            grad_head = grad_mixed[:, cols]
            grad_weights = dot_nt(grad_head, r.kv[s, 1, :, cols])
            inner = jnp.sum(weights * grad_weights, axis=-1, keepdims=True)
            grad_scores = (weights * (grad_weights - inner)).astype(LOW)
            grad_k.append(scale * dot_tn(grad_scores, queries[:, cols]))
            grad_v.append(dot_tn(weights.astype(LOW), grad_head))
            grad_q.append(scale * dot_nn(grad_scores, r.kv[s, 0, :, cols]))
        r.dkv_all[0] = jnp.concatenate(grad_k, axis=-1)
        r.dkv_all[1] = jnp.concatenate(grad_v, axis=-1)
        grad_q = jnp.concatenate(grad_q, axis=-1).astype(LOW)
        r.dqkv[s, 0] = grad_q.reshape(r.dqkv.shape[2:])
        r.norm_part[s, 7:8, :head_width] = column_sum(grad_q)

    def join_keys(s):
        @pl.when(c == 1)
        def _():
            r.dkv_out[s] = r.dkv_all[:, 0:local].astype(LOW)
            dkv_copy(s).start()

        @pl.when(c == 0)
        def _():
            dkv_copy(s).wait_recv()
            r.dkv_all[:, 0:local] += r.dkv_in[s].astype(F32)

        for which in range(2):
            joined = r.dkv_all[which, my_half].astype(LOW)
            r.dqkv[s, 1 + which] = joined.reshape(r.dqkv.shape[2:])
            if which == 1:
                r.norm_part[s, 7:8, half_width : half_width + head_width] = column_sum(joined)

    def leave_back(s):
        product = dot_nn(flat(r.dqkv.at[s, 0]), r.wq[s, 0:head_width])
        for which in range(1, 3):
            weight = r.wq[s, which * head_width : (which + 1) * head_width]
            product = product + dot_nn(flat(r.dqkv.at[s, which]), weight)
        scatter_all(s, 3, product)

    @on_owner
    def finish_back(s, j):
        grad = scatter_sum(s, 3, j)
        xhat = r.xhat1[s, j]
        result = r.middle[j] + standard_back(
            grad * r.small[s, 0:1], xhat, r.inv1[s, j, :, 0:1]
        )
        r.upstream[j] = result.astype(LOW)
        keep_rows(r.grad_low, s, j, result.astype(LOW))
        r.norm_part[s, 0:1] += column_sum(grad * xhat)
        r.norm_part[s, 1:2] += column_sum(grad)

    for j in streams:
        turn(lines - 1, j)

    def backward(index, _):
        s = lines - 1 - index
        for j in streams:
            feed_back(s, j)
        rows_start(UPS, s)
        rows_start(GPRE, s)

        @pl.when(index < 2)
        def _():
            forward_rows(lines - 2 + index)

        @pl.when(index == lines - 1)
        def _():
            share(ACT)
            share(MIX)

        for j in streams:
            between_back(s, j)
        for j in streams:
            mixed_back(s, j)
        attend_line_back(s)
        scatter_free(s, 3)
        join_keys(s)
        rows_start(BRN, s)
        leave_back(s)
        rows_start(DQKV, s)
        for j in streams:
            finish_back(s, j)

            @pl.when(s > 0)
            def _():
                turn(s - 1, j)

        norm_start(s)
        home_start(grad_home, s)
        return 0

    lax.fori_loop(0, lines, backward, 0)

    share(GPRE)
    share(DQKV)

    drain(r.norm_all, r.norm_r)
    slot = c * chips + t
    norm_sum = r.norm_all[0]
    for line in range(1, lines):
        norm_sum = norm_sum + r.norm_all[line]
    r.ends[slot] = norm_sum

    def ends_copy(step):
        core, chip = step // chips, step % chips
        view = r.ends.at[slot]
        return remote(
            view,
            view,
            r.ends_s.at[step - 1],
            r.ends_r,
            seq=(c + core) % 2,
            tensor=(t + chip) % chips,
        )

    for step in range(1, 2 * chips):
        ends_copy(step).start()

    for kind, buffer in enumerate((r.nrm, r.nmlp, r.ups, r.brn)):
        for j in streams:
            scatter_sent(0, kind, j)

            @pl.when(middle_chip)
            def _():
                gather_sent(buffer, 0, kind, j)

    for index in range(ACT):
        drain(all_rows[index], r.rows_r.at[index])
    for index in range(ACT, 8):
        share_copy(index, 1 - c).wait_recv()
        share_copy(index, c).wait_send()
    drain(r.acts, r.out_r)
    drain(r.grads, r.grad_r)
    drain(r.ends.at[0 : 2 * chips - 1], r.ends_r)
    for step in range(1, 2 * chips):
        ends_copy(step).wait_send()
    for step in range(1, lines):
        small_copy(step - 1, (a + step) % lines, a).wait_send()
        count_copy(step - 1, (a + step) % lines, a).wait_send()
    for p in range(4):
        for which, line in enumerate((beside(a), above(a))):
            first_hop(p, a, line, which).wait_send()

    @pl.when(end_chip)
    def _():
        first_copy().wait_send()

    def sent(s, _):
        home_sent(out_home, s)
        home_sent(grad_home, s)

        @pl.when(a != s)
        def _():
            norm_copy(s).wait_send()

        @pl.when(c == 0)
        def _():
            kv_copy(s).wait_send()

        @pl.when(c == 1)
        def _():
            dkv_copy(s).wait_send()

        for index in range(8):
            rows_sent(index, s)
        for p in range(4):

            @pl.when((a == beside(s)) | (a == above(s)))
            def _():
                second_hop(p, s, 0).wait_send()

            @pl.when(a != s)
            def _():
                core_hop(p, s, c).wait_send()

        return 0

    lax.fori_loop(0, lines, sent, 0)


def relay_call(inputs, cotangent, lengths, chosen, singles, weights):
    lines = lax.axis_size("section")
    chips = lax.axis_size("tensor")
    rows, buckets, width = inputs.shape[1:]
    local, total, half = rows * chips, 2 * rows * chips, width // 2
    head_width, units = weights["wo_in"].shape[0], weights["wp_in"].shape[0]
    heads = head_width // HDIM
    stream = local // STREAMS
    peers, owned = chips - 1, stream // 2
    vmem, dma = pltpu.VMEM, pltpu.SemaphoreType.DMA
    operands = dict(
        inputs=inputs,
        cotangent=cotangent,
        lengths=lengths,
        chosen=chosen,
        **singles,
        **weights,
    )

    def space(name):
        if name in weights:
            return pl.ANY
        return pltpu.SMEM if operands[name] is lengths else pltpu.VMEM

    sums = dict(
        acts=((lines, rows, width), LOW),
        grads=((lines, rows, width), LOW),
        ends=((2 * chips, 8, width), F32),
    )
    gathered = dict(
        all_nrm=((lines, 2, STREAMS, stream, half), LOW),
        all_nmlp=((lines, 2, STREAMS, stream, half), LOW),
        all_ups=((lines, 2, STREAMS, stream, half), LOW),
        all_brn=((lines, 2, STREAMS, stream, half), LOW),
        all_act=((lines, 2, STREAMS, stream, units), LOW),
        all_gpre=((lines, 2, STREAMS, stream, units), LOW),
        all_mix=((lines, 2, STREAMS, stream, head_width), LOW),
        all_dqkv=((lines, 2, 3, STREAMS, stream, head_width), LOW),
    )
    outputs = dict(**sums, **gathered)
    scratch = dict(
        wq=vmem((lines,) + weights["wq_in"].shape, LOW),
        wo=vmem((lines,) + weights["wo_in"].shape, LOW),
        wf=vmem((lines,) + weights["wf_in"].shape, LOW),
        wp=vmem((lines,) + weights["wp_in"].shape, LOW),
        small_own=vmem((8, width), F32),
        small=vmem((lines, 8, width), F32),
        count_own=vmem((lines, 8, total), F32),
        count=vmem((lines, 8, total), F32),
        hidden=vmem((STREAMS, owned, width), F32),
        middle=vmem((STREAMS, owned, width), F32),
        upstream=vmem((STREAMS, owned, width), LOW),
        first_out=vmem((2, rows, width), LOW),
        first_in=vmem((2, rows, width), LOW),
        xhat1=vmem((lines, STREAMS, owned, width), F32),
        inv1=vmem((lines, STREAMS, owned, 128), F32),
        xhat2=vmem((lines, STREAMS, owned, width), F32),
        inv2=vmem((lines, STREAMS, owned, 128), F32),
        nrm=vmem((lines, STREAMS, stream, width), LOW),
        nmlp=vmem((lines, STREAMS, stream, width), LOW),
        ups=vmem((lines, STREAMS, stream, width), LOW),
        brn=vmem((lines, STREAMS, stream, width), LOW),
        act=vmem((lines, STREAMS, stream, units), LOW),
        gpre=vmem((lines, STREAMS, stream, units), LOW),
        slope=vmem((lines, STREAMS, stream, units), F32),
        mix=vmem((lines, STREAMS, stream, head_width), LOW),
        qry=vmem((lines, STREAMS, stream, head_width), LOW),
        gmix=vmem((STREAMS, stream, head_width), LOW),
        dqkv=vmem((lines, 3, STREAMS, stream, head_width), LOW),
        kv=vmem((lines, 2, total, head_width), LOW),
        soft=vmem((lines, heads, local, total), F32),
        near=vmem((STREAMS, stream, total), F32),
        dkv_all=vmem((2, total, head_width), F32),
        dkv_out=vmem((lines, 2, local, head_width), LOW),
        dkv_in=vmem((lines, 2, local, head_width), LOW),
        part=vmem((4, STREAMS, stream, width), LOW),
        arrived=vmem((lines, 4, STREAMS, peers, owned, width), LOW),
        out_low=vmem((lines, 2, rows, width), LOW),
        grad_low=vmem((lines, 2, rows, width), LOW),
        norm_part=vmem((lines, 8, width), F32),
        norm_all=vmem((lines, 8, width), F32),
        w_first_s=dma((4, 2)),
        w_first_r=dma((lines, 4)),
        w_second_s=dma((lines, 4)),
        w_second_r=dma((lines, 4, 2)),
        w_core_s=dma((lines, 4)),
        w_core_r=dma((lines, 4)),
        w_own=dma((4,)),
        small_s=dma((lines - 1,)),
        small_r=dma((lines,)),
        count_s=dma((lines - 1,)),
        count_r=dma((lines,)),
        ag_s=dma((4, STREAMS, peers)),
        ag_r=dma((4, STREAMS, peers)),
        rs_s=dma((4, STREAMS, peers)),
        rs_r=dma((4, STREAMS, peers)),
        kv_s=dma((lines,)),
        kv_r=dma((lines,)),
        dkv_s=dma((lines,)),
        dkv_r=dma((lines,)),
        rows_s=dma((8, lines, 2)),
        rows_r=dma((8,)),
        share_s=dma((4,)),
        share_r=dma((4,)),
        first_s=dma,
        first_r=dma,
        out_s=dma((lines, 2)),
        out_r=dma,
        grad_s=dma((lines, 2)),
        grad_r=dma,
        norm_s=dma((lines,)),
        norm_r=dma,
        ends_s=dma((2 * chips - 1,)),
        ends_r=dma,
    )
    names = tuple(operands) + tuple(outputs) + tuple(scratch)
    results = pl.pallas_call(
        functools.partial(relay_kernel, names),
        out_shape=[jax.ShapeDtypeStruct(shape, kind) for shape, kind in outputs.values()],
        in_specs=[pl.BlockSpec(memory_space=space(name)) for name in operands],
        out_specs=[
            pl.BlockSpec(memory_space=pl.ANY if name in gathered else pltpu.VMEM)
            for name in outputs
        ],
        scratch_shapes=list(scratch.values()),
        compiler_params=pltpu.CompilerParams(
            collective_id=0, has_side_effects=True, vmem_limit_bytes=60 * 2**20
        ),
        name="relay",
    )(*operands.values())
    return dict(zip(outputs, results))


def weights_kernel(names, *refs):
    r = types.SimpleNamespace(**dict(zip(names, refs)))
    step = pl.program_id(0)
    micro_count, rows, buckets, width = r.activations.shape
    chips, units, head_width = r.ends.shape[0] // 2, r.all_act.shape[-1], r.all_mix.shape[-1]

    @pl.when(step == 0)
    def _():
        sums = r.ends[0]
        for other in range(1, 2 * chips):
            sums = sums + r.ends[other]
        singles = (r.ln1_gain, r.ln1_shift, r.ln2_gain, r.ln2_shift, r.b_out, r.b_proj)
        for place, single in enumerate(singles):
            single[...] = sums[place : place + 1]
        for chip in range(chips):
            both = r.ends[chip] + r.ends[chips + chip]
            r.b_fc[:, chip * units : (chip + 1) * units] = both[6:7, :units]
            here = slice(chip * head_width, (chip + 1) * head_width)
            r.b_qv[0:1, here] = both[7:8, :head_width]
            r.b_qv[1:2, here] = both[7:8, width // 2 : width // 2 + head_width]
        for target, source in ((r.activations, r.acts), (r.in_grads, r.grads)):
            for micro in range(micro_count):
                rows_of = [
                    source[micro * buckets + bucket].astype(F32)[:, None, :]
                    for bucket in range(buckets)
                ]
                target[micro] = jnp.concatenate(rows_of, axis=1).astype(LOW)
        for target in (r.w_qkv, r.w_out, r.w_fc, r.w_proj):
            target[...] = jnp.zeros_like(target)

    def rows_of_sequence(ref):
        return ref[0].reshape(2 * chips * rows, ref.shape[-1])

    nrm, nmlp, ups, brn, act, gpre, mix = (
        rows_of_sequence(ref)
        for ref in (r.all_nrm, r.all_nmlp, r.all_ups, r.all_brn, r.all_act, r.all_gpre, r.all_mix)
    )
    r.w_proj[...] += dot_tn(act, ups)
    r.w_fc[...] += dot_tn(nmlp, gpre)
    r.w_out[...] += dot_tn(mix, brn)
    for which in range(3):
        grad = r.all_dqkv[0, :, which].reshape(2 * chips * rows, head_width)
        r.w_qkv[which] += dot_tn(grad, nrm)


def weights_call(relayed, inputs_shape, head_width, units):
    lines = lax.axis_size("section")
    chips = lax.axis_size("tensor")
    width = inputs_shape[-1]
    half = width // 2
    outputs = dict(
        activations=(inputs_shape, LOW),
        in_grads=(inputs_shape, LOW),
        ln1_gain=((1, width), F32),
        ln1_shift=((1, width), F32),
        w_qkv=((3, head_width, half), F32),
        b_qv=((2, width), F32),
        w_out=((head_width, half), F32),
        b_out=((1, width), F32),
        ln2_gain=((1, width), F32),
        ln2_shift=((1, width), F32),
        w_fc=((half, units), F32),
        b_fc=((1, chips * units), F32),
        w_proj=((units, half), F32),
        b_proj=((1, width), F32),
    )

    def spec(array):
        if len(array.shape) < 5:
            return pl.BlockSpec(array.shape, lambda step: (0,) * len(array.shape))
        return pl.BlockSpec(
            (1,) + array.shape[1:], lambda step: (step,) + (0,) * (len(array.shape) - 1)
        )

    def whole(shape):
        return pl.BlockSpec(shape, lambda step: (0,) * len(shape))

    return pl.pallas_call(
        functools.partial(weights_kernel, tuple(relayed) + tuple(outputs)),
        out_shape=[jax.ShapeDtypeStruct(shape, kind) for shape, kind in outputs.values()],
        grid=(lines,),
        in_specs=[spec(array) for array in relayed.values()],
        out_specs=[whole(shape) for shape, _ in outputs.values()],
        compiler_params=pltpu.CompilerParams(vmem_limit_bytes=60 * 2**20),
        name="weight_gradients",
    )(*relayed.values())


def on_line(
    inputs,
    cotangent,
    lengths,
    chosen,
    ln1_gain,
    ln1_shift,
    w_qkv,
    b_qv,
    w_out,
    b_out,
    ln2_gain,
    ln2_shift,
    w_fc,
    b_fc,
    w_proj,
    b_proj,
):
    head_width, units = w_out.shape[1], w_fc.shape[2]
    singles = dict(
        ln1_gain=ln1_gain,
        ln1_shift=ln1_shift,
        ln2_gain=ln2_gain,
        ln2_shift=ln2_shift,
        b_out=b_out,
        b_proj=b_proj,
        b_fc=b_fc,
        b_qv=b_qv[0],
    )
    weights = dict(
        wq_in=jnp.swapaxes(w_qkv[0], 1, 2).reshape(-1, inputs.shape[-1]),
        wo_in=w_out[0],
        wf_in=w_fc[0],
        wp_in=w_proj[0],
    )
    picks = chosen.reshape((-1,) + chosen.shape[-2:])
    relayed = relay_call(inputs, cotangent, lengths, picks, singles, weights)
    results = list(weights_call(relayed, inputs.shape, head_width, units))
    results[4] = jnp.swapaxes(results[4], 1, 2)
    vectors = (2, 3, 7, 8, 9, 11, 13)
    return tuple(
        result if place in vectors else result[None] for place, result in enumerate(results)
    )


def fits_lines(mesh):
    return mesh.shape["section"] == 4 and mesh.shape["seq"] == 2 and mesh.shape["tensor"] == 4


def solution(mesh):
    placed = (
        P(None, ("seq", "tensor"), None, None),
        P(None, ("seq", "tensor"), None, None),
        P(),
        P("section", None, None, "tensor", "seq", None),
        P("section", None),
        P("section", None),
        P("section", None, None, "tensor"),
        P("section", None, "tensor"),
        P("section", "tensor", None),
        P("section", None),
        P("section", None),
        P("section", None),
        P("section", None, "tensor"),
        P("section", "tensor"),
        P("section", "tensor", None),
        P("section", None),
    )
    return jax.shard_map(
        on_line if fits_lines(mesh) else on_device,
        mesh=mesh,
        in_specs=placed,
        out_specs=(
            P("section", None, ("seq", "tensor"), None, None),
            P("section", None, ("seq", "tensor"), None, None),
            P("section", None),
            P("section", None),
            P("section", None, "seq", "tensor"),
            P("section", None, None),
            P("section", "tensor", "seq"),
            P("section", None),
            P("section", None),
            P("section", None),
            P("section", "seq", "tensor"),
            P("section", None),
            P("section", "tensor", "seq"),
            P("section", None),
        ),
        check_vma=False,
    )
```

```python
import functools
import types

import jax
import jax.numpy as jnp
from jax import lax
from jax.experimental import pallas as pl
from jax.experimental.pallas import tpu as pltpu
from jax.sharding import PartitionSpec as P

HDIM = 64
WIN = 64
QB = 64
KSEL = 64


NORM_EPS = 1e-05
MASKED = -1000000000.0


def from_behind(value, axis, steps):
    count = lax.axis_size(axis)
    first, last = (max(0, -steps), min(count, count - steps))
    return lax.ppermute(value, axis, [(source, source + steps) for source in range(first, last)])


def layer_norm(values, gain, shift):
    average = jnp.mean(values, axis=-1, keepdims=True)
    centred = values - average
    variance = jnp.mean(centred * centred, axis=-1, keepdims=True)
    return centred * lax.rsqrt(variance + NORM_EPS) * gain + shift


def gelu_tanh(values):
    return (
        0.5
        * values
        * (1.0 + jnp.tanh(0.7978845608028654 * (values + 0.044715 * values * values * values)))
    )


def gather_rows(row_block):
    return lax.all_gather(row_block, "tensor", axis=0, tiled=True)


def scatter_product(left_rows, weight, formula):
    return lax.psum_scatter(
        jnp.einsum(formula, left_rows, weight, preferred_element_type=jnp.float32).astype(
            jnp.bfloat16
        ),
        "tensor",
        scatter_dimension=0,
        tiled=True,
    ).astype(jnp.float32)


def near_slabs(full_rows, seq_start, seq_first, length_local):
    buckets = full_rows.shape[1]
    heads_local = full_rows.shape[2] // HDIM
    blocks = length_local // QB
    earlier = lax.dynamic_slice_in_dim(full_rows, jnp.maximum(seq_start - WIN, 0), WIN, 0)
    earlier = jnp.where(seq_first, jnp.zeros_like(earlier), earlier)
    local_part = lax.dynamic_slice_in_dim(full_rows, seq_start, length_local, 0)
    segment = jnp.concatenate([earlier, local_part], 0).reshape(
        length_local + WIN, buckets, heads_local, HDIM
    )
    return jnp.concatenate(
        [
            segment[offset_index * QB : offset_index * QB + length_local].reshape(
                blocks, QB, buckets, heads_local, HDIM
            )
            for offset_index in range(WIN // QB + 1)
        ],
        1,
    )


def far_rows(full_rows, flat_index):
    total_rows, buckets, feature_width = full_rows.shape
    heads_local = feature_width // HDIM
    return jnp.take(full_rows.reshape(total_rows * buckets * heads_local, HDIM), flat_index, axis=0)


def key_geometry(chosen_now, seq_start, blocks):
    buckets, heads_local = (chosen_now.shape[0], chosen_now.shape[1])
    bucket_ids = lax.broadcasted_iota(jnp.int32, chosen_now.shape, 0)
    head_ids = lax.broadcasted_iota(jnp.int32, chosen_now.shape, 1)
    flat_index = (chosen_now * buckets + bucket_ids) * heads_local + head_ids
    block_start = seq_start + QB * lax.broadcasted_iota(jnp.int32, (blocks, 1, 1), 0)
    query_ids = lax.broadcasted_iota(jnp.int32, (1, QB, 1), 1)
    key_ids = lax.broadcasted_iota(jnp.int32, (1, 1, WIN + QB), 2)
    distance = query_ids + WIN - key_ids
    near_ok = (distance >= 0) & (distance < WIN) & (block_start + key_ids - WIN >= 0)
    far_ok = chosen_now + WIN <= block_start.reshape(1, 1, blocks, 1)
    near_mask = jnp.broadcast_to(
        near_ok[:, None, None], (blocks, buckets, heads_local, QB, WIN + QB)
    )
    far_mask = jnp.broadcast_to(
        jnp.transpose(far_ok, (2, 0, 1, 3))[:, :, :, None, :],
        (blocks, buckets, heads_local, QB, KSEL),
    )
    return (flat_index, jnp.concatenate([near_mask, far_mask], -1))


def attention_setup(queries, key_rows, value_rows, chosen_now, seq_start, seq_first):
    length_local, buckets, feature_width = queries.shape
    heads_local = feature_width // HDIM
    blocks = length_local // QB
    query_blocks = queries.reshape(blocks, QB, buckets, heads_local, HDIM)
    flat_index, key_mask = key_geometry(chosen_now, seq_start, blocks)
    near_keys = near_slabs(key_rows, seq_start, seq_first, length_local)
    near_values = near_slabs(value_rows, seq_start, seq_first, length_local)
    far_keys = far_rows(key_rows, flat_index)
    far_values = far_rows(value_rows, flat_index)
    near_scores = jnp.einsum(
        "bqnhe,btnhe->bnhqt", query_blocks, near_keys, preferred_element_type=jnp.float32
    )
    far_scores = jnp.einsum(
        "bqnhe,nhbke->bnhqk", query_blocks, far_keys, preferred_element_type=jnp.float32
    )
    scores = jnp.where(
        key_mask, HDIM ** (-0.5) * jnp.concatenate([near_scores, far_scores], -1), MASKED
    )
    return (query_blocks, near_keys, near_values, far_keys, far_values, flat_index, scores)


def attend(queries, key_rows, value_rows, chosen_now, seq_start, seq_first):
    query_blocks, near_keys, near_values, far_keys, far_values, flat_index, scores = (
        attention_setup(queries, key_rows, value_rows, chosen_now, seq_start, seq_first)
    )
    span = WIN + QB
    row_top = jnp.max(scores, -1, keepdims=True)
    exp_terms = jnp.exp(scores - row_top)
    row_total = jnp.sum(exp_terms, -1, keepdims=True)
    softmax_low = (exp_terms / row_total).astype(jnp.bfloat16)
    near_part = jnp.einsum(
        "bnhqt,btnhe->bqnhe",
        softmax_low[..., :span],
        near_values,
        preferred_element_type=jnp.float32,
    )
    far_part = jnp.einsum(
        "bnhqk,nhbke->bqnhe",
        softmax_low[..., span:],
        far_values,
        preferred_element_type=jnp.float32,
    )
    return ((near_part + far_part).reshape(queries.shape), row_top + jnp.log(row_total))


def spread_back(near_grad, far_grad, flat_index, seq_start, seq_first, total_rows):
    blocks, span, buckets, heads_local, head_size = near_grad.shape
    length_local = blocks * QB
    feature_width = heads_local * head_size
    segment = jnp.zeros((length_local + WIN, buckets, heads_local, head_size), jnp.float32)
    for offset_index in range(WIN // QB + 1):
        piece = near_grad[:, offset_index * QB : (offset_index + 1) * QB].reshape(
            length_local, buckets, heads_local, head_size
        )
        segment = segment.at[offset_index * QB : offset_index * QB + length_local].add(piece)
    full_rows = jnp.zeros((total_rows * buckets * heads_local, head_size), jnp.float32)
    full_rows = full_rows.at[flat_index.reshape(-1)].add(far_grad.reshape(-1, head_size))
    full_rows = full_rows.reshape(total_rows, buckets, feature_width)
    local_part = segment[WIN:].reshape(length_local, buckets, feature_width)
    earlier = jnp.where(seq_first, 0.0, segment[:WIN].reshape(WIN, buckets, feature_width))
    full_rows = lax.dynamic_update_slice_in_dim(
        full_rows,
        lax.dynamic_slice_in_dim(full_rows, seq_start, length_local, 0) + local_part,
        seq_start,
        0,
    )
    earlier_start = jnp.maximum(seq_start - WIN, 0)
    full_rows = lax.dynamic_update_slice_in_dim(
        full_rows,
        lax.dynamic_slice_in_dim(full_rows, earlier_start, WIN, 0) + earlier,
        earlier_start,
        0,
    )
    return full_rows


def attend_back(
    queries, key_rows, value_rows, chosen_now, seq_start, seq_first, log_total, grad_mixed
):
    query_blocks, near_keys, near_values, far_keys, far_values, flat_index, scores = (
        attention_setup(queries, key_rows, value_rows, chosen_now, seq_start, seq_first)
    )
    span = WIN + QB
    score_scale = HDIM ** (-0.5)
    grad_blocks = grad_mixed.reshape(query_blocks.shape)
    weights_full = jnp.exp(scores - log_total)
    softmax_low = weights_full.astype(jnp.bfloat16)
    grad_near_weights = jnp.einsum(
        "bqnhe,btnhe->bnhqt", grad_blocks, near_values, preferred_element_type=jnp.float32
    )
    grad_far_weights = jnp.einsum(
        "bqnhe,nhbke->bnhqk", grad_blocks, far_values, preferred_element_type=jnp.float32
    )
    grad_weights = jnp.concatenate([grad_near_weights, grad_far_weights], -1)
    row_dot = jnp.sum(weights_full * grad_weights, -1, keepdims=True)
    grad_scores = (weights_full * (grad_weights - row_dot)).astype(jnp.bfloat16)
    grad_near, grad_far = (grad_scores[..., :span], grad_scores[..., span:])
    grad_queries = score_scale * (
        jnp.einsum("bnhqt,btnhe->bqnhe", grad_near, near_keys, preferred_element_type=jnp.float32)
        + jnp.einsum("bnhqk,nhbke->bqnhe", grad_far, far_keys, preferred_element_type=jnp.float32)
    )
    near_key_grad = score_scale * jnp.einsum(
        "bnhqt,bqnhe->btnhe", grad_near, query_blocks, preferred_element_type=jnp.float32
    )
    far_key_grad = score_scale * jnp.einsum(
        "bnhqk,bqnhe->nhbke", grad_far, query_blocks, preferred_element_type=jnp.float32
    )
    near_value_grad = jnp.einsum(
        "bnhqt,bqnhe->btnhe",
        softmax_low[..., :span],
        grad_blocks,
        preferred_element_type=jnp.float32,
    )
    far_value_grad = jnp.einsum(
        "bnhqk,bqnhe->nhbke",
        softmax_low[..., span:],
        grad_blocks,
        preferred_element_type=jnp.float32,
    )
    total_rows = key_rows.shape[0]
    key_grad = spread_back(
        near_key_grad, far_key_grad, flat_index, seq_start, seq_first, total_rows
    )
    value_grad = spread_back(
        near_value_grad, far_value_grad, flat_index, seq_start, seq_first, total_rows
    )
    return (grad_queries.reshape(queries.shape), key_grad, value_grad)


def forward_pass(hidden, params, chosen_now, query_mask, seq_start, seq_first, finish):
    (
        ln1_gain,
        ln1_shift,
        w_qkv,
        b_qv,
        w_out,
        b_out,
        ln2_gain,
        ln2_shift,
        w_fc,
        b_fc,
        w_proj,
        b_proj,
    ) = params
    hidden_wide = hidden.astype(jnp.float32)
    normed_all = gather_rows(layer_norm(hidden_wide, ln1_gain, ln1_shift).astype(jnp.bfloat16))
    projected = jnp.einsum("pnd,jdc->jpnc", normed_all, w_qkv, preferred_element_type=jnp.float32)
    queries = (projected[0] + b_qv[0]).astype(jnp.bfloat16)
    key_rows, value_rows = (
        lax.all_gather(projected[1].astype(jnp.bfloat16), "seq", axis=0, tiled=True),
        lax.all_gather((projected[2] + b_qv[1]).astype(jnp.bfloat16), "seq", axis=0, tiled=True),
    )
    attended, log_total = attend(queries, key_rows, value_rows, chosen_now, seq_start, seq_first)
    mixed_rows = (attended * query_mask[:, :, None]).astype(jnp.bfloat16)
    middle = hidden_wide + scatter_product(mixed_rows, w_out, "pnc,cd->pnd") + b_out
    normed_mlp = gather_rows(layer_norm(middle, ln2_gain, ln2_shift).astype(jnp.bfloat16))
    pre_active = (
        jnp.einsum("pnd,df->pnf", normed_mlp, w_fc, preferred_element_type=jnp.float32) + b_fc
    )
    active = gelu_tanh(pre_active).astype(jnp.bfloat16)
    if not finish:
        return (
            normed_all,
            queries,
            key_rows,
            value_rows,
            log_total,
            mixed_rows,
            middle,
            normed_mlp,
            pre_active,
            active,
        )
    output = (middle + scatter_product(active, w_proj, "pnf,fd->pnd") + b_proj).astype(jnp.bfloat16)
    return (output, (key_rows, value_rows))


def backward_pass(hidden, upstream, params, chosen_now, query_mask, seq_start, seq_first):
    (
        ln1_gain,
        ln1_shift,
        w_qkv,
        b_qv,
        w_out,
        b_out,
        ln2_gain,
        ln2_shift,
        w_fc,
        b_fc,
        w_proj,
        b_proj,
    ) = params
    (
        normed_all,
        queries,
        key_rows,
        value_rows,
        log_total,
        mixed_rows,
        middle,
        normed_mlp,
        pre_active,
        active,
    ) = forward_pass(hidden, params, chosen_now, query_mask, seq_start, seq_first, False)
    upstream_all = gather_rows(upstream)
    grad_w_proj = jnp.einsum(
        "pnf,pnd->fd", active, upstream_all, preferred_element_type=jnp.float32
    )
    grad_b_proj = jnp.sum(upstream.astype(jnp.float32), axis=(0, 1))
    grad_active = jnp.einsum(
        "pnd,fd->pnf", upstream_all, w_proj, preferred_element_type=jnp.float32
    )
    unused_value, gelu_pull = jax.vjp(gelu_tanh, pre_active)
    grad_pre = gelu_pull(grad_active)[0].astype(jnp.bfloat16)
    grad_w_fc = jnp.einsum("pnd,pnf->df", normed_mlp, grad_pre, preferred_element_type=jnp.float32)
    grad_b_fc = jnp.sum(grad_pre.astype(jnp.float32), axis=(0, 1))
    grad_normed_mlp = scatter_product(grad_pre, w_fc, "pnf,df->pnd")
    unused_norm, second_pull = jax.vjp(layer_norm, middle, ln2_gain, ln2_shift)
    grad_mid_norm, grad_ln2_gain, grad_ln2_shift = second_pull(grad_normed_mlp)
    grad_middle = upstream.astype(jnp.float32) + grad_mid_norm
    grad_branch = grad_middle.astype(jnp.bfloat16)
    grad_b_out = jnp.sum(grad_branch.astype(jnp.float32), axis=(0, 1))
    branch_all = gather_rows(grad_branch)
    grad_w_out = jnp.einsum(
        "pnc,pnd->cd", mixed_rows, branch_all, preferred_element_type=jnp.float32
    )
    grad_mixed = jnp.einsum(
        "pnd,cd->pnc", branch_all, w_out, preferred_element_type=jnp.float32
    ).astype(jnp.bfloat16) * query_mask[:, :, None].astype(jnp.bfloat16)
    grad_queries, key_grad_all, value_grad_all = attend_back(
        queries, key_rows, value_rows, chosen_now, seq_start, seq_first, log_total, grad_mixed
    )
    key_grad, value_grad = (
        lax.psum_scatter(
            key_grad_all.astype(jnp.bfloat16), "seq", scatter_dimension=0, tiled=True
        ).astype(jnp.float32),
        lax.psum_scatter(
            value_grad_all.astype(jnp.bfloat16), "seq", scatter_dimension=0, tiled=True
        ).astype(jnp.float32),
    )
    grad_project = jnp.stack(
        [
            grad_queries.astype(jnp.bfloat16),
            key_grad.astype(jnp.bfloat16),
            value_grad.astype(jnp.bfloat16),
        ],
        2,
    )
    grad_w_qkv = jnp.einsum(
        "pnd,pnjc->jdc", normed_all, grad_project, preferred_element_type=jnp.float32
    )
    grad_b_qv = jnp.sum(grad_project[:, :, 0::2].astype(jnp.float32), axis=(0, 1))
    grad_normed = scatter_product(grad_project, w_qkv, "pnjc,jdc->pnd")
    unused_first, first_pull = jax.vjp(layer_norm, hidden.astype(jnp.float32), ln1_gain, ln1_shift)
    grad_in_norm, grad_ln1_gain, grad_ln1_shift = first_pull(grad_normed)
    grad_hidden = (grad_middle + grad_in_norm).astype(jnp.bfloat16)
    block_grads = (
        grad_ln1_gain,
        grad_ln1_shift,
        grad_w_qkv,
        grad_b_qv,
        grad_w_out,
        grad_b_out,
        grad_ln2_gain,
        grad_ln2_shift,
        grad_w_fc,
        grad_b_fc,
        grad_w_proj,
        grad_b_proj,
    )
    return (grad_hidden, block_grads)


def on_device(
    inputs,
    cotangent,
    lengths,
    chosen,
    ln1_gain,
    ln1_shift,
    w_qkv,
    b_qv,
    w_out,
    b_out,
    ln2_gain,
    ln2_shift,
    w_fc,
    b_fc,
    w_proj,
    b_proj,
):
    params = tuple(
        (
            weight_array[0]
            for weight_array in (
                ln1_gain,
                ln1_shift,
                w_qkv,
                b_qv,
                w_out,
                b_out,
                ln2_gain,
                ln2_shift,
                w_fc,
                b_fc,
                w_proj,
                b_proj,
            )
        )
    )
    section_index = lax.axis_index("section")
    section_count = lax.axis_size("section")
    seq_index = lax.axis_index("seq")
    tensor_index = lax.axis_index("tensor")
    tensor_count = lax.axis_size("tensor")
    micro_count, rows_local, buckets, feature_width = inputs.shape
    length_local = rows_local * tensor_count
    heads_width = w_qkv.shape[-1]
    seq_start = seq_index * length_local
    seq_first = seq_index == 0
    positions = seq_start + lax.broadcasted_iota(jnp.int32, (micro_count, length_local, buckets), 1)
    mask_all = (positions < lengths[:, None, :]).astype(jnp.float32)
    mask_rows = lax.dynamic_slice_in_dim(mask_all, tensor_index * rows_local, rows_local, 1)
    step_count = micro_count + section_count - 1
    chosen_section = chosen[0]
    received = jnp.zeros((rows_local, buckets, feature_width), jnp.bfloat16)
    stored = jnp.zeros((micro_count, rows_local, buckets, feature_width), jnp.bfloat16)
    outputs = jnp.zeros_like(stored)
    for step_index in range(step_count):
        micro_index = step_index - section_index
        running = (micro_index >= 0) & (micro_index < micro_count)
        slot_index = jnp.clip(micro_index, 0, micro_count - 1)
        block_in = jnp.where(
            section_index == 0, lax.dynamic_index_in_dim(inputs, slot_index, 0, False), received
        )
        chosen_now = lax.dynamic_index_in_dim(chosen_section, slot_index, 0, False)
        query_mask = lax.dynamic_index_in_dim(mask_all, slot_index, 0, False)
        result, key_pair = forward_pass(
            block_in, params, chosen_now, query_mask, seq_start, seq_first, True
        )
        stored = jnp.where(
            running, lax.dynamic_update_index_in_dim(stored, block_in, slot_index, 0), stored
        )
        outputs = jnp.where(
            running, lax.dynamic_update_index_in_dim(outputs, result, slot_index, 0), outputs
        )
        received = from_behind(result, "section", 1)
    back_received = jnp.zeros((rows_local, buckets, feature_width), jnp.bfloat16)
    in_grads = jnp.zeros_like(stored)
    totals = None
    for step_index in range(step_count):
        micro_index = step_index - (section_count - 1 - section_index)
        running = (micro_index >= 0) & (micro_index < micro_count)
        slot_index = jnp.clip(micro_index, 0, micro_count - 1)
        chosen_now = lax.dynamic_index_in_dim(chosen_section, slot_index, 0, False)
        query_mask = lax.dynamic_index_in_dim(mask_all, slot_index, 0, False)
        local_mask = lax.dynamic_index_in_dim(mask_rows, slot_index, 0, False)
        top_grad = (
            lax.dynamic_index_in_dim(cotangent, slot_index, 0, False).astype(jnp.float32)
            * local_mask[:, :, None]
        ).astype(jnp.bfloat16)
        upstream = jnp.where(section_index == section_count - 1, top_grad, back_received)
        hidden = lax.dynamic_index_in_dim(stored, slot_index, 0, False)
        grad_hidden, block_grads = backward_pass(
            hidden, upstream, params, chosen_now, query_mask, seq_start, seq_first
        )
        block_grads = tuple(
            (jnp.where(running, grad_part, jnp.zeros_like(grad_part)) for grad_part in block_grads)
        )
        totals = (
            block_grads
            if step_index == 0
            else tuple(
                (total_part + grad_part for total_part, grad_part in zip(totals, block_grads))
            )
        )
        in_grads = jnp.where(
            running, lax.dynamic_update_index_in_dim(in_grads, grad_hidden, slot_index, 0), in_grads
        )
        back_received = from_behind(grad_hidden, "section", -1)
    (
        sum_ln1_gain,
        sum_ln1_shift,
        sum_w_qkv,
        sum_b_qv,
        sum_w_out,
        sum_b_out,
        sum_ln2_gain,
        sum_ln2_shift,
        sum_w_fc,
        sum_b_fc,
        sum_w_proj,
        sum_b_proj,
    ) = totals
    part_qkv, part_out, part_fc, part_proj = (
        lax.psum_scatter(
            sum_w_qkv.astype(jnp.bfloat16), "seq", scatter_dimension=1, tiled=True
        ).astype(jnp.float32),
        lax.psum_scatter(
            sum_w_out.astype(jnp.bfloat16), "seq", scatter_dimension=1, tiled=True
        ).astype(jnp.float32),
        lax.psum_scatter(
            sum_w_fc.astype(jnp.bfloat16), "seq", scatter_dimension=0, tiled=True
        ).astype(jnp.float32),
        lax.psum_scatter(
            sum_w_proj.astype(jnp.bfloat16), "seq", scatter_dimension=1, tiled=True
        ).astype(jnp.float32),
    )
    bias_qv = lax.dynamic_update_slice_in_dim(
        jnp.zeros((2, feature_width), jnp.float32), sum_b_qv, tensor_index * heads_width, 1
    )
    units_local = sum_b_fc.shape[0]
    bias_fc = lax.dynamic_update_slice_in_dim(
        jnp.zeros((units_local * tensor_count,), jnp.float32),
        sum_b_fc,
        tensor_index * units_local,
        0,
    )
    small_sums = lax.psum(
        (
            sum_ln1_gain,
            sum_ln1_shift,
            bias_qv,
            sum_b_out,
            sum_ln2_gain,
            sum_ln2_shift,
            bias_fc,
            sum_b_proj,
        ),
        ("seq", "tensor"),
    )
    return (
        outputs[None],
        in_grads[None],
        small_sums[0][None],
        small_sums[1][None],
        part_qkv[None],
        small_sums[2][None],
        part_out[None],
        small_sums[3][None],
        small_sums[4][None],
        small_sums[5][None],
        part_fc[None],
        small_sums[6][None],
        part_proj[None],
        small_sums[7][None],
    )


STREAMS = 2
NRM, NMLP, UPS, BRN, ACT, GPRE, MIX, DQKV = range(8)
F32 = jnp.float32
LOW = jnp.bfloat16
MESH_ID = pl.DeviceIdType.MESH


def dot_nn(left, right):
    return lax.dot_general(left, right, (((1,), (0,)), ((), ())), preferred_element_type=F32)


def dot_nt(left, right):
    return lax.dot_general(left, right, (((1,), (1,)), ((), ())), preferred_element_type=F32)


def dot_tn(left, right):
    return lax.dot_general(left, right, (((0,), (0,)), ((), ())), preferred_element_type=F32)


def standard(rows):
    centred = rows - jnp.mean(rows, axis=-1, keepdims=True)
    scale = lax.rsqrt(jnp.mean(centred * centred, axis=-1, keepdims=True) + NORM_EPS)
    return centred * scale, scale


def standard_back(grad, xhat, scale):
    inner = jnp.mean(grad * xhat, axis=-1, keepdims=True)
    return scale * (grad - jnp.mean(grad, axis=-1, keepdims=True) - xhat * inner)


def column_sum(rows):
    return jnp.sum(rows.astype(F32), axis=0, keepdims=True)


def relay_kernel(names, *refs):
    r = types.SimpleNamespace(**dict(zip(names, refs)))
    a, c, t = (lax.axis_index(name) for name in ("section", "seq", "tensor"))
    lines = lax.axis_size("section")
    chips = lax.axis_size("tensor")
    rows, buckets, width = r.inputs.shape[1:]
    half_width = width // 2
    local = rows * chips
    total = 2 * local
    stream_rows = local // STREAMS
    head_width = r.wo_in.shape[0]
    heads = head_width // HDIM
    blocks = local // QB
    units = r.wp_in.shape[0]
    scale = HDIM ** (-0.5)
    streams = range(STREAMS)

    def remote(src, dst, send, recv, **target):
        return pltpu.make_async_remote_copy(
            src_ref=src,
            dst_ref=dst,
            send_sem=send,
            recv_sem=recv,
            device_id=target,
            device_id_type=MESH_ID,
        )

    def drain(ref, sem):
        pltpu.make_async_copy(ref, ref, sem).wait()

    def row_block(index, size):
        return pl.ds(pl.multiple_of(index * size, size), size)

    near_chip = t + 1 - 2 * (t % 2)
    over_chip = (t + 2) % 4
    across_chip = 3 - t
    middle_chip = (t == 1) | (t == 2)
    end_chip = (t == 0) | (t == 3)
    owned = stream_rows // 2
    mine = row_block(t - 1, owned)
    my_half = row_block(c, local)

    barrier = pltpu.get_barrier_semaphore()
    for core in range(2):
        for step in range(1, chips):
            there = {"tensor": (t + step) % chips, "seq": core}
            pl.semaphore_signal(barrier, inc=1, device_id=there, device_id_type=MESH_ID)
        for step in range(1, lines):
            there = {"section": (a + step) % lines, "seq": core}
            pl.semaphore_signal(barrier, inc=1, device_id=there, device_id_type=MESH_ID)
    for step in range(1, lines):
        there = {"section": (a + step) % lines, "tensor": near_chip}
        pl.semaphore_signal(barrier, inc=1, device_id=there, device_id_type=MESH_ID)
    pl.semaphore_signal(barrier, inc=1, device_id={"seq": 1 - c}, device_id_type=MESH_ID)
    pl.semaphore_wait(barrier, 2 * (chips - 1) + 3 * (lines - 1) + 1)

    def beside(s):
        return s + 1 - 2 * (s % 2)

    def above(s):
        return (s + 2) % 4

    def store(p):
        return (r.wq, r.wo, r.wf, r.wp)[p]

    def source(p):
        return (r.wq_in, r.wo_in, r.wf_in, r.wp_in)[p]

    def height(p):
        return source(p).shape[0]

    def core_half(p, s, core):
        return store(p).at[s, row_block(core, height(p) // 2)]

    def first_hop(p, s, neighbour, which):
        return remote(
            source(p).at[row_block(c, height(p) // 2)],
            core_half(p, s, c),
            r.w_first_s.at[p, which],
            r.w_first_r.at[s, p],
            section=neighbour,
        )

    def second_hop(p, s, which):
        view = store(p).at[s, row_block(2 * c + which, height(p) // 4)]
        return remote(
            view, view, r.w_second_s.at[s, p], r.w_second_r.at[s, p, which], section=3 - s
        )

    def core_hop(p, s, core):
        view = core_half(p, s, core)
        return remote(view, view, r.w_core_s.at[s, p], r.w_core_r.at[s, p], seq=1 - c)

    def own_copy(p):
        return pltpu.make_async_copy(source(p), store(p).at[a], r.w_own.at[p])

    def pass_on(s, p, which):
        line = (beside(s), above(s))[which]

        @pl.when(a == line)
        def _():
            first_hop(p, s, line, which).wait_recv()
            second_hop(p, s, which).start()
            core_hop(p, s, c).start()

    def pass_all(s, pieces):
        for p in pieces:
            for which in range(2):
                pass_on(s, p, which)

    def pass_far(s, p):
        @pl.when(a == 3 - s)
        def _():
            second_hop(p, s, 0).wait_recv()
            second_hop(p, s, 1).wait_recv()
            core_hop(p, s, c).start()

    def need(s, p):
        @pl.when(s == 0)
        def _():
            if p < 2:
                pass_all(0, (p,))
            pass_far(0, p)

        @pl.when(a == s)
        def _():
            own_copy(p).wait()

        @pl.when(a != s)
        def _():
            core_hop(p, s, 1 - c).wait_recv()

    def small_copy(step, line, slot):
        return remote(
            r.small_own, r.small.at[slot], r.small_s.at[step], r.small_r.at[slot], section=line
        )

    def count_copy(step, line, slot):
        return remote(
            r.count_own.at[line],
            r.count.at[slot],
            r.count_s.at[step],
            r.count_r.at[slot],
            section=line,
        )

    singles = (r.ln1_gain, r.ln1_shift, r.ln2_gain, r.ln2_shift, r.b_out, r.b_proj)
    for place, single in enumerate(singles):
        r.small_own[place : place + 1] = single[...]
    r.small_own[6:7, :units] = r.b_fc[...]
    r.small_own[7:8, :head_width] = r.b_qv[0:1]
    r.small_own[7:8, half_width : half_width + head_width] = r.b_qv[1:2]
    for step in range(1, lines):
        small_copy(step - 1, (a + step) % lines, a).start()
    for p in range(4):
        for which, line in enumerate((beside(a), above(a))):
            first_hop(p, a, line, which).start()
    for p in range(4):
        own_copy(p).start()
    r.small[a] = r.small_own[...]

    def place_of(index):
        inside = index % local
        stream, left = inside // stream_rows, inside % stream_rows
        first = (index // local) * local + (left // owned) * (local // 2)
        return first + stream * owned + left % owned

    def iota(shape, dimension):
        return lax.broadcasted_iota(jnp.int32, shape, dimension)

    square = jnp.where(iota((KSEL, KSEL), 0) == iota((KSEL, KSEL), 1), 1.0, 0.0).astype(LOW)
    position = place_of(iota((KSEL, total), 1)).astype(F32)
    for pair in range(lines * heads):
        line, head = pair // heads, pair % heads
        columns = dot_nt(square, r.chosen[pair].astype(F32).astype(LOW))
        for block in range(blocks):
            pick = head * blocks + block
            r.count_own[line, pick : pick + 1, :] = jnp.sum(
                jnp.where(columns[:, block : block + 1] == position, 1.0, 0.0),
                axis=0,
                keepdims=True,
            )
    for step in range(1, lines):
        count_copy(step - 1, (a + step) % lines, a).start()
    r.count[a] = r.count_own[a]

    NEAR, OVER, ACROSS = range(3)

    def gather(buffer, s, kind, j, owner, target, slot):
        view = buffer.at[s, j, row_block(owner - 1, owned)]
        return remote(
            view, view, r.ag_s.at[kind, j, slot], r.ag_r.at[kind, j, slot], tensor=target
        )

    def used_before(s, kind):
        return s > 0 if kind < 2 else s < lines - 1

    def gather_start(buffer, s, kind, j):
        @pl.when(used_before(s, kind))
        def _():
            gather_sent(buffer, s, kind, j)

        gather(buffer, s, kind, j, t, over_chip, OVER).start()
        gather(buffer, s, kind, j, t, across_chip, ACROSS).start()
        gather(buffer, s, kind, j, t, near_chip, NEAR).start()

    def gather_wait(buffer, s, kind, j):
        @pl.when(middle_chip)
        def _():
            gather(buffer, s, kind, j, across_chip, across_chip, ACROSS).wait_recv()

        @pl.when(end_chip)
        def _():
            gather(buffer, s, kind, j, near_chip, near_chip, NEAR).wait_recv()
            gather(buffer, s, kind, j, over_chip, over_chip, OVER).wait_recv()

    def gather_sent(buffer, s, kind, j):
        gather(buffer, s, kind, j, t, over_chip, OVER).wait_send()
        gather(buffer, s, kind, j, t, across_chip, ACROSS).wait_send()
        gather(buffer, s, kind, j, t, near_chip, NEAR).wait_send()

    def scatter(s, kind, j, owner, slot):
        return remote(
            r.part.at[kind, j, row_block(owner - 1, owned)],
            r.arrived.at[s, kind, j, slot],
            r.rs_s.at[kind, j, slot],
            r.rs_r.at[kind, j, slot],
            tensor=owner,
        )

    def scatter_start(s, kind, j, product):
        @pl.when(used_before(s, kind))
        def _():
            scatter_sent(s, kind, j)

        r.part[kind, j] = product.astype(LOW)
        scatter_send(s, kind, j)

    def scatter_all(s, kind, product):
        r.part[kind] = product.astype(LOW).reshape(r.part.shape[1:])
        for j in streams:
            scatter_send(s, kind, j)

    def scatter_free(s, kind):
        @pl.when(used_before(s, kind))
        def _():
            for j in streams:
                scatter_sent(s, kind, j)

    def scatter_send(s, kind, j):
        @pl.when(end_chip)
        def _():
            scatter(s, kind, j, over_chip, OVER).start()
            scatter(s, kind, j, near_chip, NEAR).start()

        @pl.when(middle_chip)
        def _():
            scatter(s, kind, j, across_chip, ACROSS).start()

    def scatter_sum(s, kind, j):
        result = r.part[kind, j, mine].astype(F32)
        for slot in (NEAR, ACROSS, OVER):
            scatter(s, kind, j, t, slot).wait_recv()
            result = result + r.arrived[s, kind, j, slot].astype(F32)
        return result

    def scatter_sent(s, kind, j):
        @pl.when(end_chip)
        def _():
            scatter(s, kind, j, over_chip, OVER).wait_send()
            scatter(s, kind, j, near_chip, NEAR).wait_send()

        @pl.when(middle_chip)
        def _():
            scatter(s, kind, j, across_chip, ACROSS).wait_send()

    own_rows = (r.nrm, r.nmlp, r.ups, r.brn, r.act, r.gpre, r.mix, r.dqkv)
    all_rows = (
        r.all_nrm,
        r.all_nmlp,
        r.all_ups,
        r.all_brn,
        r.all_act,
        r.all_gpre,
        r.all_mix,
        r.all_dqkv,
    )

    def rows_copy(index, s, same, stays=False):
        core = c if same else 1 - c
        src = own_rows[index].at[s]
        dst = all_rows[index].at[a, c]
        if index <= BRN:
            src = src.at[:, :, row_block(core, half_width)]
        recv = r.rows_r.at[index]
        if stays:
            return pltpu.make_async_copy(src, dst, recv)
        if same:
            return remote(src, dst, r.rows_s.at[index, s, 0], recv, section=s)
        return remote(src, dst, r.rows_s.at[index, s, 1], recv, section=s, seq=1 - c)

    def rows_start(index, s):
        @pl.when(a == s)
        def _():
            rows_copy(index, s, True, True).start()

        @pl.when(a != s)
        def _():
            rows_copy(index, s, True).start()

        if index <= BRN:
            rows_copy(index, s, False).start()

    def forward_rows(s):
        for index in (NRM, MIX, NMLP, ACT):
            rows_start(index, s)

    def forward_rows_at(step):
        for delay in range(1, 4):
            s = step - delay
            line = (None, beside(s), above(s), 3 - s)[delay]
            sends = a == line
            if delay == 1:
                sends = sends | (a == s)

            @pl.when(sends & (s >= 0) & (s < lines))
            def _():
                forward_rows(s)

    def rows_sent(index, s):
        @pl.when(a != s)
        def _():
            rows_copy(index, s, True).wait_send()

        if index <= BRN:
            rows_copy(index, s, False).wait_send()

    def share_copy(index, core):
        view = all_rows[index].at[:, core]
        return remote(view, view, r.share_s.at[index - ACT], r.share_r.at[index - ACT], seq=1 - c)

    def share(index):
        drain(all_rows[index].at[:, c], r.rows_r.at[index])
        share_copy(index, c).start()

    def norm_copy(s):
        return remote(
            r.norm_part.at[s], r.norm_all.at[a], r.norm_s.at[s], r.norm_r, section=s
        )

    def norm_start(s):
        @pl.when(a == s)
        def _():
            pltpu.make_async_copy(r.norm_part.at[s], r.norm_all.at[a], r.norm_r).start()

        @pl.when(a != s)
        def _():
            norm_copy(s).start()

    def home_copy(what, s, chip):
        src, dst, send, recv = what
        return remote(
            src.at[s, chip % 2],
            dst.at[a],
            send.at[s, chip % 2],
            recv,
            section=s,
            tensor=chip,
        )

    def home_start(what, s):
        src, dst, send, recv = what

        @pl.when(middle_chip & (a == s))
        def _():
            pltpu.make_async_copy(src.at[s, t % 2], dst.at[a], recv).start()

        @pl.when(middle_chip & (a != s))
        def _():
            home_copy(what, s, t).start()

        @pl.when(middle_chip)
        def _():
            home_copy(what, s, near_chip).start()

    def home_sent(what, s):
        @pl.when(middle_chip & (a != s))
        def _():
            home_copy(what, s, t).wait_send()

        @pl.when(middle_chip)
        def _():
            home_copy(what, s, near_chip).wait_send()

    out_home = (r.out_low, r.acts, r.out_s, r.out_r)
    grad_home = (r.grad_low, r.grads, r.grad_s, r.grad_r)

    length = r.lengths[a // buckets, a % buckets]
    key = place_of(iota((stream_rows, total), 1))
    for j in streams:
        query = place_of(c * local + j * stream_rows + iota((stream_rows, total), 0))
        r.near[j] = jnp.where((query >= key) & (query - key < WIN), 1.0, 0.0)
    key_row = place_of(iota((1, total), 1))

    def row_mask(place):
        return jnp.where(place < length, 1.0, 0.0)

    def multiplicity(s, head):
        far = []
        for block in range(blocks):
            pick = head * blocks + block
            limit = (c * blocks + block) * QB - WIN
            counted = jnp.where(key_row <= limit, r.count[s, pick : pick + 1, :], 0.0)
            far.append(jnp.broadcast_to(counted, (stream_rows // blocks, total)))
        return flat(r.near) + jnp.concatenate(far * STREAMS, axis=0)

    def flat(ref):
        return ref[...].reshape(local, ref.shape[-1])

    def head_cols(head):
        return slice(head * HDIM, (head + 1) * HDIM)

    def kv_copy(s):
        view = r.kv.at[s, :, 0:local]
        return remote(view, view, r.kv_s.at[s], r.kv_r.at[s], seq=1 - c)

    def dkv_copy(s):
        return remote(r.dkv_out.at[s], r.dkv_in.at[s], r.dkv_s.at[s], r.dkv_r.at[s], seq=1 - c)

    def own_sequence(ref):
        both = ref[a // buckets].astype(F32)
        picked = both[:, 0, :]
        for bucket in range(1, buckets):
            picked = jnp.where(a % buckets == bucket, both[:, bucket, :], picked)
        return picked

    def own_part(j):
        chip, first = (j * owned) // rows, (j * owned) % rows
        return chip, slice(first, first + owned)

    def first_copy():
        return remote(r.first_out, r.first_in, r.first_s, r.first_r, tensor=near_chip)

    own_place = c * local + t * rows + iota((rows, 1), 0)
    r.first_out[0] = own_sequence(r.inputs).astype(LOW)
    r.first_out[1] = (own_sequence(r.cotangent) * row_mask(own_place)).astype(LOW)
    r.norm_part[...] = jnp.zeros_like(r.norm_part)

    @pl.when(c == 0)
    def _():
        r.kv[:, :, local:total] = jnp.zeros((lines, 2, local, head_width), LOW)


    @pl.when(end_chip)
    def _():
        first_copy().start()

    @pl.when(middle_chip)
    def _():
        first_copy().wait_recv()
        for which in range(2):
            here, beside_it = r.first_out[which].astype(F32), r.first_in[which].astype(F32)
            lower = jnp.where(t % 2 == 0, here, beside_it)
            upper = jnp.where(t % 2 == 0, beside_it, here)
            for j in streams:
                chip, part = own_part(j)
                own_block = (lower, upper)[chip][part]
                if which == 0:
                    r.hidden[j] = own_block
                else:
                    r.upstream[j] = own_block.astype(LOW)

    def on_owner(stage):
        def run(s, j):
            @pl.when(middle_chip)
            def _():
                stage(s, j)

        return run

    def keep_rows(target, s, j, result):
        chip, part = own_part(j)
        target[s, chip, part] = result

    @on_owner
    def enter(s, j):
        xhat, inverse = standard(r.hidden[j])
        r.xhat1[s, j] = xhat
        r.inv1[s, j] = jnp.broadcast_to(inverse, (owned, 128))
        r.nrm[s, j, mine] = (xhat * r.small[s, 0:1] + r.small[s, 1:2]).astype(LOW)
        gather_start(r.nrm, s, 0, j)

    def project(s, j):
        gather_wait(r.nrm, s, 0, j)
        normed = r.nrm[s, j]
        place = row_block(c * STREAMS + j, stream_rows)
        bias_v = r.small[s, 7:8, half_width : half_width + head_width]
        key_rows = dot_nt(normed, r.wq[s, head_width : 2 * head_width])
        value_rows = dot_nt(normed, r.wq[s, 2 * head_width : 3 * head_width]) + bias_v
        r.kv[s, 0, place] = key_rows.astype(LOW)
        r.kv[s, 1, place] = value_rows.astype(LOW)

    def ask(s, j):
        queries = dot_nt(r.nrm[s, j], r.wq[s, 0:head_width]) + r.small[s, 7:8, :head_width]
        r.qry[s, j] = queries.astype(LOW)

    def attend_line(s):
        mixed = []
        queries = flat(r.qry.at[s])
        for head in range(heads):
            cols = head_cols(head)
            times = multiplicity(s, head)
            scores = scale * dot_nt(queries[:, cols], r.kv[s, 0, :, cols])
            scores = jnp.where(times > 0.0, scores, MASKED)
            top = jnp.max(scores, axis=-1, keepdims=True)
            terms = times * jnp.exp(scores - top)
            weights = terms / jnp.sum(terms, axis=-1, keepdims=True)
            r.soft[s, head] = weights
            mixed.append(dot_nn(weights.astype(LOW), r.kv[s, 1, :, cols]))
        mask = row_mask(place_of(c * local + iota((local, 1), 0)))
        mixed = (jnp.concatenate(mixed, axis=-1) * mask).astype(LOW)
        r.mix[s] = mixed.reshape(r.mix.shape[1:])
        scatter_all(s, 0, dot_nn(mixed, r.wo[s]))

    @on_owner
    def between(s, j):
        middle = r.hidden[j] + scatter_sum(s, 0, j) + r.small[s, 4:5]
        r.middle[j] = middle
        xhat, inverse = standard(middle)
        r.xhat2[s, j] = xhat
        r.inv2[s, j] = jnp.broadcast_to(inverse, (owned, 128))
        r.nmlp[s, j, mine] = (xhat * r.small[s, 2:3] + r.small[s, 3:4]).astype(LOW)
        gather_start(r.nmlp, s, 1, j)

    def feed(s, j):
        gather_wait(r.nmlp, s, 1, j)
        before = dot_nn(r.nmlp[s, j], r.wf[s]) + r.small[s, 6:7, :units]
        bend = jnp.tanh(0.7978845608028654 * (before + 0.044715 * before * before * before))
        r.act[s, j] = (0.5 * before * (1.0 + bend)).astype(LOW)
        r.slope[s, j] = 0.5 * (1.0 + bend) + 0.5 * before * (1.0 - bend * bend) * (
            0.7978845608028654 * (1.0 + 3 * 0.044715 * before * before)
        )


    def leave_feed(s, j):
        scatter_start(s, 1, j, dot_nn(r.act[s, j], r.wp[s]))

    @on_owner
    def finish(s, j):
        result = r.middle[j] + scatter_sum(s, 1, j) + r.small[s, 5:6]
        keep_rows(r.out_low, s, j, result.astype(LOW))
        r.hidden[j] = result.astype(LOW).astype(F32)

    def small_ready(s):
        @pl.when(a != s)
        def _():
            small_copy(0, a, s).wait_recv()

    small_ready(0)
    for j in streams:
        enter(0, j)

    def forward(s, _):
        need(s, 0)
        for j in streams:
            project(s, j)

        @pl.when(c == 0)
        def _():
            kv_copy(s).start()

        forward_rows_at(s)
        for j in streams:
            ask(s, j)

        @pl.when(a != s)
        def _():
            count_copy(0, a, s).wait_recv()

        @pl.when(c == 1)
        def _():
            kv_copy(s).wait_recv()

        need(s, 1)
        scatter_free(s, 0)
        attend_line(s)

        @pl.when(s == 0)
        def _():
            pass_all(0, (2,))
            for later in range(1, lines):
                pass_all(later, (0, 1, 2))

        @pl.when(s == 1)
        def _():
            pass_far(1, 2)
            pass_far(1, 3)
            for later in range(2, lines):
                for p in range(4):
                    pass_far(later, p)

        for j in streams:
            between(s, j)
        @pl.when(s == 0)
        def _():
            for later in range(lines):
                pass_all(later, (3,))

        need(s, 2)
        for j in streams:
            feed(s, j)
            if j == 0:
                need(s, 3)
            leave_feed(s, j)


        @pl.when(s + 1 < lines)
        def _():
            small_ready(s + 1)

        for j in streams:
            finish(s, j)

            @pl.when(s + 1 < lines)
            def _():
                enter(s + 1, j)

        home_start(out_home, s)

        @pl.when(s == 0)
        def _():
            pass_far(1, 0)
            pass_far(1, 1)

        return 0

    lax.fori_loop(0, lines, forward, 0)

    @on_owner
    def turn(s, j):
        upstream = r.upstream[j]
        r.ups[s, j, mine] = upstream
        gather_start(r.ups, s, 2, j)
        r.norm_part[s, 5:6] += column_sum(upstream)

    def feed_back(s, j):
        gather_wait(r.ups, s, 2, j)
        grad_pre = (dot_nt(r.ups[s, j], r.wp[s]) * r.slope[s, j]).astype(LOW)
        r.gpre[s, j] = grad_pre
        scatter_start(s, 2, j, dot_nt(grad_pre, r.wf[s]))
        r.norm_part[s, 6:7, :units] += column_sum(grad_pre)

    @on_owner
    def between_back(s, j):
        grad = scatter_sum(s, 2, j)
        xhat = r.xhat2[s, j]
        upstream = r.upstream[j].astype(F32)
        grad_middle = upstream + standard_back(
            grad * r.small[s, 2:3], xhat, r.inv2[s, j, :, 0:1]
        )
        r.middle[j] = grad_middle
        branch = grad_middle.astype(LOW)
        r.brn[s, j, mine] = branch
        gather_start(r.brn, s, 3, j)
        r.norm_part[s, 2:3] += column_sum(grad * xhat)
        r.norm_part[s, 3:4] += column_sum(grad)
        r.norm_part[s, 4:5] += column_sum(branch)

    def mixed_back(s, j):
        gather_wait(r.brn, s, 3, j)
        place = place_of(c * local + j * stream_rows + iota((stream_rows, 1), 0))
        r.gmix[j] = (dot_nt(r.brn[s, j], r.wo[s]) * row_mask(place)).astype(LOW)

    def attend_line_back(s):
        grad_q, grad_k, grad_v = [], [], []
        grad_mixed, queries = flat(r.gmix), flat(r.qry.at[s])
        for head in range(heads):
            cols = head_cols(head)
            weights = r.soft[s, head]
            grad_head = grad_mixed[:, cols]
            grad_weights = dot_nt(grad_head, r.kv[s, 1, :, cols])
            inner = jnp.sum(weights * grad_weights, axis=-1, keepdims=True)
            grad_scores = (weights * (grad_weights - inner)).astype(LOW)
            grad_k.append(scale * dot_tn(grad_scores, queries[:, cols]))
            grad_v.append(dot_tn(weights.astype(LOW), grad_head))
            grad_q.append(scale * dot_nn(grad_scores, r.kv[s, 0, :, cols]))
        r.dkv_all[0] = jnp.concatenate(grad_k, axis=-1)
        r.dkv_all[1] = jnp.concatenate(grad_v, axis=-1)
        grad_q = jnp.concatenate(grad_q, axis=-1).astype(LOW)
        r.dqkv[s, 0] = grad_q.reshape(r.dqkv.shape[2:])
        r.norm_part[s, 7:8, :head_width] = column_sum(grad_q)

    def join_keys(s):
        @pl.when(c == 1)
        def _():
            r.dkv_out[s] = r.dkv_all[:, 0:local].astype(LOW)
            dkv_copy(s).start()

        @pl.when(c == 0)
        def _():
            dkv_copy(s).wait_recv()
            r.dkv_all[:, 0:local] += r.dkv_in[s].astype(F32)

        for which in range(2):
            joined = r.dkv_all[which, my_half].astype(LOW)
            r.dqkv[s, 1 + which] = joined.reshape(r.dqkv.shape[2:])
            if which == 1:
                r.norm_part[s, 7:8, half_width : half_width + head_width] = column_sum(joined)

    def leave_back(s):
        product = dot_nn(flat(r.dqkv.at[s, 0]), r.wq[s, 0:head_width])
        for which in range(1, 3):
            weight = r.wq[s, which * head_width : (which + 1) * head_width]
            product = product + dot_nn(flat(r.dqkv.at[s, which]), weight)
        scatter_all(s, 3, product)

    @on_owner
    def finish_back(s, j):
        grad = scatter_sum(s, 3, j)
        xhat = r.xhat1[s, j]
        result = r.middle[j] + standard_back(
            grad * r.small[s, 0:1], xhat, r.inv1[s, j, :, 0:1]
        )
        r.upstream[j] = result.astype(LOW)
        keep_rows(r.grad_low, s, j, result.astype(LOW))
        r.norm_part[s, 0:1] += column_sum(grad * xhat)
        r.norm_part[s, 1:2] += column_sum(grad)

    for j in streams:
        turn(lines - 1, j)

    def backward(index, _):
        s = lines - 1 - index
        for j in streams:
            feed_back(s, j)
        for j in streams:
            between_back(s, j)
        @pl.when((a != 3 - s) | (s == 0))
        def _():
            rows_start(UPS, s)
            rows_start(GPRE, s)

        @pl.when(index > 0)
        def _():
            rows_start(BRN, s + 1)
            rows_start(DQKV, s + 1)

        @pl.when((index > 0) & (a == 2 - s))
        def _():
            rows_start(UPS, s + 1)
            rows_start(GPRE, s + 1)

        forward_rows_at(lines + index)

        @pl.when(index == lines - 1)
        def _():
            share(ACT)
            share(MIX)

        for j in streams:
            mixed_back(s, j)
        attend_line_back(s)
        scatter_free(s, 3)
        join_keys(s)
        leave_back(s)

        @pl.when(s == 0)
        def _():
            rows_start(BRN, 0)
            rows_start(DQKV, 0)

        for j in streams:
            finish_back(s, j)

            @pl.when(s > 0)
            def _():
                turn(s - 1, j)

        norm_start(s)
        home_start(grad_home, s)
        return 0

    lax.fori_loop(0, lines, backward, 0)

    share(GPRE)
    share(DQKV)

    drain(r.norm_all, r.norm_r)
    slot = c * chips + t
    norm_sum = r.norm_all[0]
    for line in range(1, lines):
        norm_sum = norm_sum + r.norm_all[line]
    r.ends[slot] = norm_sum

    def ends_copy(step):
        core, chip = step // chips, step % chips
        view = r.ends.at[slot]
        return remote(
            view,
            view,
            r.ends_s.at[step - 1],
            r.ends_r,
            seq=(c + core) % 2,
            tensor=(t + chip) % chips,
        )

    for step in range(1, 2 * chips):
        ends_copy(step).start()

    for kind, buffer in enumerate((r.nrm, r.nmlp, r.ups, r.brn)):
        for j in streams:
            scatter_sent(0, kind, j)

            @pl.when(middle_chip)
            def _():
                gather_sent(buffer, 0, kind, j)

    for index in range(ACT):
        drain(all_rows[index], r.rows_r.at[index])
    for index in range(ACT, 8):
        share_copy(index, 1 - c).wait_recv()
        share_copy(index, c).wait_send()
    drain(r.acts, r.out_r)
    drain(r.grads, r.grad_r)
    drain(r.ends.at[0 : 2 * chips - 1], r.ends_r)
    for step in range(1, 2 * chips):
        ends_copy(step).wait_send()
    for step in range(1, lines):
        small_copy(step - 1, (a + step) % lines, a).wait_send()
        count_copy(step - 1, (a + step) % lines, a).wait_send()
    for p in range(4):
        for which, line in enumerate((beside(a), above(a))):
            first_hop(p, a, line, which).wait_send()

    @pl.when(end_chip)
    def _():
        first_copy().wait_send()

    def sent(s, _):
        home_sent(out_home, s)
        home_sent(grad_home, s)

        @pl.when(a != s)
        def _():
            norm_copy(s).wait_send()

        @pl.when(c == 0)
        def _():
            kv_copy(s).wait_send()

        @pl.when(c == 1)
        def _():
            dkv_copy(s).wait_send()

        for index in range(8):
            rows_sent(index, s)
        for p in range(4):

            @pl.when((a == beside(s)) | (a == above(s)))
            def _():
                second_hop(p, s, 0).wait_send()

            @pl.when(a != s)
            def _():
                core_hop(p, s, c).wait_send()

        return 0

    lax.fori_loop(0, lines, sent, 0)


def relay_call(inputs, cotangent, lengths, chosen, singles, weights):
    lines = lax.axis_size("section")
    chips = lax.axis_size("tensor")
    rows, buckets, width = inputs.shape[1:]
    local, total, half = rows * chips, 2 * rows * chips, width // 2
    head_width, units = weights["wo_in"].shape[0], weights["wp_in"].shape[0]
    heads = head_width // HDIM
    stream = local // STREAMS
    peers, owned = chips - 1, stream // 2
    vmem, dma = pltpu.VMEM, pltpu.SemaphoreType.DMA
    operands = dict(
        inputs=inputs,
        cotangent=cotangent,
        lengths=lengths,
        chosen=chosen,
        **singles,
        **weights,
    )

    def space(name):
        if name in weights:
            return pl.ANY
        return pltpu.SMEM if operands[name] is lengths else pltpu.VMEM

    sums = dict(
        acts=((lines, rows, width), LOW),
        grads=((lines, rows, width), LOW),
        ends=((2 * chips, 8, width), F32),
    )
    gathered = dict(
        all_nrm=((lines, 2, STREAMS, stream, half), LOW),
        all_nmlp=((lines, 2, STREAMS, stream, half), LOW),
        all_ups=((lines, 2, STREAMS, stream, half), LOW),
        all_brn=((lines, 2, STREAMS, stream, half), LOW),
        all_act=((lines, 2, STREAMS, stream, units), LOW),
        all_gpre=((lines, 2, STREAMS, stream, units), LOW),
        all_mix=((lines, 2, STREAMS, stream, head_width), LOW),
        all_dqkv=((lines, 2, 3, STREAMS, stream, head_width), LOW),
    )
    outputs = dict(**sums, **gathered)
    scratch = dict(
        wq=vmem((lines,) + weights["wq_in"].shape, LOW),
        wo=vmem((lines,) + weights["wo_in"].shape, LOW),
        wf=vmem((lines,) + weights["wf_in"].shape, LOW),
        wp=vmem((lines,) + weights["wp_in"].shape, LOW),
        small_own=vmem((8, width), F32),
        small=vmem((lines, 8, width), F32),
        count_own=vmem((lines, 8, total), F32),
        count=vmem((lines, 8, total), F32),
        hidden=vmem((STREAMS, owned, width), F32),
        middle=vmem((STREAMS, owned, width), F32),
        upstream=vmem((STREAMS, owned, width), LOW),
        first_out=vmem((2, rows, width), LOW),
        first_in=vmem((2, rows, width), LOW),
        xhat1=vmem((lines, STREAMS, owned, width), F32),
        inv1=vmem((lines, STREAMS, owned, 128), F32),
        xhat2=vmem((lines, STREAMS, owned, width), F32),
        inv2=vmem((lines, STREAMS, owned, 128), F32),
        nrm=vmem((lines, STREAMS, stream, width), LOW),
        nmlp=vmem((lines, STREAMS, stream, width), LOW),
        ups=vmem((lines, STREAMS, stream, width), LOW),
        brn=vmem((lines, STREAMS, stream, width), LOW),
        act=vmem((lines, STREAMS, stream, units), LOW),
        gpre=vmem((lines, STREAMS, stream, units), LOW),
        slope=vmem((lines, STREAMS, stream, units), F32),
        mix=vmem((lines, STREAMS, stream, head_width), LOW),
        qry=vmem((lines, STREAMS, stream, head_width), LOW),
        gmix=vmem((STREAMS, stream, head_width), LOW),
        dqkv=vmem((lines, 3, STREAMS, stream, head_width), LOW),
        kv=vmem((lines, 2, total, head_width), LOW),
        soft=vmem((lines, heads, local, total), F32),
        near=vmem((STREAMS, stream, total), F32),
        dkv_all=vmem((2, total, head_width), F32),
        dkv_out=vmem((lines, 2, local, head_width), LOW),
        dkv_in=vmem((lines, 2, local, head_width), LOW),
        part=vmem((4, STREAMS, stream, width), LOW),
        arrived=vmem((lines, 4, STREAMS, peers, owned, width), LOW),
        out_low=vmem((lines, 2, rows, width), LOW),
        grad_low=vmem((lines, 2, rows, width), LOW),
        norm_part=vmem((lines, 8, width), F32),
        norm_all=vmem((lines, 8, width), F32),
        w_first_s=dma((4, 2)),
        w_first_r=dma((lines, 4)),
        w_second_s=dma((lines, 4)),
        w_second_r=dma((lines, 4, 2)),
        w_core_s=dma((lines, 4)),
        w_core_r=dma((lines, 4)),
        w_own=dma((4,)),
        small_s=dma((lines - 1,)),
        small_r=dma((lines,)),
        count_s=dma((lines - 1,)),
        count_r=dma((lines,)),
        ag_s=dma((4, STREAMS, peers)),
        ag_r=dma((4, STREAMS, peers)),
        rs_s=dma((4, STREAMS, peers)),
        rs_r=dma((4, STREAMS, peers)),
        kv_s=dma((lines,)),
        kv_r=dma((lines,)),
        dkv_s=dma((lines,)),
        dkv_r=dma((lines,)),
        rows_s=dma((8, lines, 2)),
        rows_r=dma((8,)),
        share_s=dma((4,)),
        share_r=dma((4,)),
        first_s=dma,
        first_r=dma,
        out_s=dma((lines, 2)),
        out_r=dma,
        grad_s=dma((lines, 2)),
        grad_r=dma,
        norm_s=dma((lines,)),
        norm_r=dma,
        ends_s=dma((2 * chips - 1,)),
        ends_r=dma,
    )
    names = tuple(operands) + tuple(outputs) + tuple(scratch)
    results = pl.pallas_call(
        functools.partial(relay_kernel, names),
        out_shape=[jax.ShapeDtypeStruct(shape, kind) for shape, kind in outputs.values()],
        in_specs=[pl.BlockSpec(memory_space=space(name)) for name in operands],
        out_specs=[
            pl.BlockSpec(memory_space=pl.ANY if name in gathered else pltpu.VMEM)
            for name in outputs
        ],
        scratch_shapes=list(scratch.values()),
        compiler_params=pltpu.CompilerParams(
            collective_id=0, has_side_effects=True, vmem_limit_bytes=60 * 2**20
        ),
        name="relay",
    )(*operands.values())
    return dict(zip(outputs, results))


def weights_kernel(names, *refs):
    r = types.SimpleNamespace(**dict(zip(names, refs)))
    step = pl.program_id(0)
    micro_count, rows, buckets, width = r.activations.shape
    chips, units, head_width = r.ends.shape[0] // 2, r.all_act.shape[-1], r.all_mix.shape[-1]

    @pl.when(step == 0)
    def _():
        sums = r.ends[0]
        for other in range(1, 2 * chips):
            sums = sums + r.ends[other]
        singles = (r.ln1_gain, r.ln1_shift, r.ln2_gain, r.ln2_shift, r.b_out, r.b_proj)
        for place, single in enumerate(singles):
            single[...] = sums[place : place + 1]
        for chip in range(chips):
            both = r.ends[chip] + r.ends[chips + chip]
            r.b_fc[:, chip * units : (chip + 1) * units] = both[6:7, :units]
            here = slice(chip * head_width, (chip + 1) * head_width)
            r.b_qv[0:1, here] = both[7:8, :head_width]
            r.b_qv[1:2, here] = both[7:8, width // 2 : width // 2 + head_width]
        for target, source in ((r.activations, r.acts), (r.in_grads, r.grads)):
            for micro in range(micro_count):
                rows_of = [
                    source[micro * buckets + bucket].astype(F32)[:, None, :]
                    for bucket in range(buckets)
                ]
                target[micro] = jnp.concatenate(rows_of, axis=1).astype(LOW)
        for target in (r.w_qkv, r.w_out, r.w_fc, r.w_proj):
            target[...] = jnp.zeros_like(target)

    def rows_of_sequence(ref):
        return ref[0].reshape(2 * chips * rows, ref.shape[-1])

    nrm, nmlp, ups, brn, act, gpre, mix = (
        rows_of_sequence(ref)
        for ref in (r.all_nrm, r.all_nmlp, r.all_ups, r.all_brn, r.all_act, r.all_gpre, r.all_mix)
    )
    r.w_proj[...] += dot_tn(act, ups)
    r.w_fc[...] += dot_tn(nmlp, gpre)
    r.w_out[...] += dot_tn(mix, brn)
    for which in range(3):
        grad = r.all_dqkv[0, :, which].reshape(2 * chips * rows, head_width)
        r.w_qkv[which] += dot_tn(grad, nrm)


def weights_call(relayed, inputs_shape, head_width, units):
    lines = lax.axis_size("section")
    chips = lax.axis_size("tensor")
    width = inputs_shape[-1]
    half = width // 2
    outputs = dict(
        activations=(inputs_shape, LOW),
        in_grads=(inputs_shape, LOW),
        ln1_gain=((1, width), F32),
        ln1_shift=((1, width), F32),
        w_qkv=((3, head_width, half), F32),
        b_qv=((2, width), F32),
        w_out=((head_width, half), F32),
        b_out=((1, width), F32),
        ln2_gain=((1, width), F32),
        ln2_shift=((1, width), F32),
        w_fc=((half, units), F32),
        b_fc=((1, chips * units), F32),
        w_proj=((units, half), F32),
        b_proj=((1, width), F32),
    )

    def spec(array):
        if len(array.shape) < 5:
            return pl.BlockSpec(array.shape, lambda step: (0,) * len(array.shape))
        return pl.BlockSpec(
            (1,) + array.shape[1:], lambda step: (step,) + (0,) * (len(array.shape) - 1)
        )

    def whole(shape):
        return pl.BlockSpec(shape, lambda step: (0,) * len(shape))

    return pl.pallas_call(
        functools.partial(weights_kernel, tuple(relayed) + tuple(outputs)),
        out_shape=[jax.ShapeDtypeStruct(shape, kind) for shape, kind in outputs.values()],
        grid=(lines,),
        in_specs=[spec(array) for array in relayed.values()],
        out_specs=[whole(shape) for shape, _ in outputs.values()],
        compiler_params=pltpu.CompilerParams(vmem_limit_bytes=60 * 2**20),
        name="weight_gradients",
    )(*relayed.values())


def on_line(
    inputs,
    cotangent,
    lengths,
    chosen,
    ln1_gain,
    ln1_shift,
    w_qkv,
    b_qv,
    w_out,
    b_out,
    ln2_gain,
    ln2_shift,
    w_fc,
    b_fc,
    w_proj,
    b_proj,
):
    head_width, units = w_out.shape[1], w_fc.shape[2]
    singles = dict(
        ln1_gain=ln1_gain,
        ln1_shift=ln1_shift,
        ln2_gain=ln2_gain,
        ln2_shift=ln2_shift,
        b_out=b_out,
        b_proj=b_proj,
        b_fc=b_fc,
        b_qv=b_qv[0],
    )
    weights = dict(
        wq_in=jnp.swapaxes(w_qkv[0], 1, 2).reshape(-1, inputs.shape[-1]),
        wo_in=w_out[0],
        wf_in=w_fc[0],
        wp_in=w_proj[0],
    )
    picks = chosen.reshape((-1,) + chosen.shape[-2:])
    relayed = relay_call(inputs, cotangent, lengths, picks, singles, weights)
    results = list(weights_call(relayed, inputs.shape, head_width, units))
    results[4] = jnp.swapaxes(results[4], 1, 2)
    vectors = (2, 3, 7, 8, 9, 11, 13)
    return tuple(
        result if place in vectors else result[None] for place, result in enumerate(results)
    )


def fits_lines(mesh):
    return mesh.shape["section"] == 4 and mesh.shape["seq"] == 2 and mesh.shape["tensor"] == 4


def solution(mesh):
    placed = (
        P(None, ("seq", "tensor"), None, None),
        P(None, ("seq", "tensor"), None, None),
        P(),
        P("section", None, None, "tensor", "seq", None),
        P("section", None),
        P("section", None),
        P("section", None, None, "tensor"),
        P("section", None, "tensor"),
        P("section", "tensor", None),
        P("section", None),
        P("section", None),
        P("section", None),
        P("section", None, "tensor"),
        P("section", "tensor"),
        P("section", "tensor", None),
        P("section", None),
    )
    return jax.shard_map(
        on_line if fits_lines(mesh) else on_device,
        mesh=mesh,
        in_specs=placed,
        out_specs=(
            P("section", None, ("seq", "tensor"), None, None),
            P("section", None, ("seq", "tensor"), None, None),
            P("section", None),
            P("section", None),
            P("section", None, "seq", "tensor"),
            P("section", None, None),
            P("section", "tensor", "seq"),
            P("section", None),
            P("section", None),
            P("section", None),
            P("section", "seq", "tensor"),
            P("section", None),
            P("section", "tensor", "seq"),
            P("section", None),
        ),
        check_vma=False,
    )
```

```python
import functools
import types

import jax
import jax.numpy as jnp
from jax import lax
from jax.experimental import pallas as pl
from jax.experimental.pallas import tpu as pltpu
from jax.sharding import PartitionSpec as P

HDIM = 64
WIN = 64
QB = 64
KSEL = 64


NORM_EPS = 1e-05
MASKED = -1000000000.0


def from_behind(value, axis, steps):
    count = lax.axis_size(axis)
    first, last = (max(0, -steps), min(count, count - steps))
    return lax.ppermute(value, axis, [(source, source + steps) for source in range(first, last)])


def layer_norm(values, gain, shift):
    average = jnp.mean(values, axis=-1, keepdims=True)
    centred = values - average
    variance = jnp.mean(centred * centred, axis=-1, keepdims=True)
    return centred * lax.rsqrt(variance + NORM_EPS) * gain + shift


def gelu_tanh(values):
    return (
        0.5
        * values
        * (1.0 + jnp.tanh(0.7978845608028654 * (values + 0.044715 * values * values * values)))
    )


def gather_rows(row_block):
    return lax.all_gather(row_block, "tensor", axis=0, tiled=True)


def scatter_product(left_rows, weight, formula):
    return lax.psum_scatter(
        jnp.einsum(formula, left_rows, weight, preferred_element_type=jnp.float32).astype(
            jnp.bfloat16
        ),
        "tensor",
        scatter_dimension=0,
        tiled=True,
    ).astype(jnp.float32)


def near_slabs(full_rows, seq_start, seq_first, length_local):
    buckets = full_rows.shape[1]
    heads_local = full_rows.shape[2] // HDIM
    blocks = length_local // QB
    earlier = lax.dynamic_slice_in_dim(full_rows, jnp.maximum(seq_start - WIN, 0), WIN, 0)
    earlier = jnp.where(seq_first, jnp.zeros_like(earlier), earlier)
    local_part = lax.dynamic_slice_in_dim(full_rows, seq_start, length_local, 0)
    segment = jnp.concatenate([earlier, local_part], 0).reshape(
        length_local + WIN, buckets, heads_local, HDIM
    )
    return jnp.concatenate(
        [
            segment[offset_index * QB : offset_index * QB + length_local].reshape(
                blocks, QB, buckets, heads_local, HDIM
            )
            for offset_index in range(WIN // QB + 1)
        ],
        1,
    )


def far_rows(full_rows, flat_index):
    total_rows, buckets, feature_width = full_rows.shape
    heads_local = feature_width // HDIM
    return jnp.take(full_rows.reshape(total_rows * buckets * heads_local, HDIM), flat_index, axis=0)


def key_geometry(chosen_now, seq_start, blocks):
    buckets, heads_local = (chosen_now.shape[0], chosen_now.shape[1])
    bucket_ids = lax.broadcasted_iota(jnp.int32, chosen_now.shape, 0)
    head_ids = lax.broadcasted_iota(jnp.int32, chosen_now.shape, 1)
    flat_index = (chosen_now * buckets + bucket_ids) * heads_local + head_ids
    block_start = seq_start + QB * lax.broadcasted_iota(jnp.int32, (blocks, 1, 1), 0)
    query_ids = lax.broadcasted_iota(jnp.int32, (1, QB, 1), 1)
    key_ids = lax.broadcasted_iota(jnp.int32, (1, 1, WIN + QB), 2)
    distance = query_ids + WIN - key_ids
    near_ok = (distance >= 0) & (distance < WIN) & (block_start + key_ids - WIN >= 0)
    far_ok = chosen_now + WIN <= block_start.reshape(1, 1, blocks, 1)
    near_mask = jnp.broadcast_to(
        near_ok[:, None, None], (blocks, buckets, heads_local, QB, WIN + QB)
    )
    far_mask = jnp.broadcast_to(
        jnp.transpose(far_ok, (2, 0, 1, 3))[:, :, :, None, :],
        (blocks, buckets, heads_local, QB, KSEL),
    )
    return (flat_index, jnp.concatenate([near_mask, far_mask], -1))


def attention_setup(queries, key_rows, value_rows, chosen_now, seq_start, seq_first):
    length_local, buckets, feature_width = queries.shape
    heads_local = feature_width // HDIM
    blocks = length_local // QB
    query_blocks = queries.reshape(blocks, QB, buckets, heads_local, HDIM)
    flat_index, key_mask = key_geometry(chosen_now, seq_start, blocks)
    near_keys = near_slabs(key_rows, seq_start, seq_first, length_local)
    near_values = near_slabs(value_rows, seq_start, seq_first, length_local)
    far_keys = far_rows(key_rows, flat_index)
    far_values = far_rows(value_rows, flat_index)
    near_scores = jnp.einsum(
        "bqnhe,btnhe->bnhqt", query_blocks, near_keys, preferred_element_type=jnp.float32
    )
    far_scores = jnp.einsum(
        "bqnhe,nhbke->bnhqk", query_blocks, far_keys, preferred_element_type=jnp.float32
    )
    scores = jnp.where(
        key_mask, HDIM ** (-0.5) * jnp.concatenate([near_scores, far_scores], -1), MASKED
    )
    return (query_blocks, near_keys, near_values, far_keys, far_values, flat_index, scores)


def attend(queries, key_rows, value_rows, chosen_now, seq_start, seq_first):
    query_blocks, near_keys, near_values, far_keys, far_values, flat_index, scores = (
        attention_setup(queries, key_rows, value_rows, chosen_now, seq_start, seq_first)
    )
    span = WIN + QB
    row_top = jnp.max(scores, -1, keepdims=True)
    exp_terms = jnp.exp(scores - row_top)
    row_total = jnp.sum(exp_terms, -1, keepdims=True)
    softmax_low = (exp_terms / row_total).astype(jnp.bfloat16)
    near_part = jnp.einsum(
        "bnhqt,btnhe->bqnhe",
        softmax_low[..., :span],
        near_values,
        preferred_element_type=jnp.float32,
    )
    far_part = jnp.einsum(
        "bnhqk,nhbke->bqnhe",
        softmax_low[..., span:],
        far_values,
        preferred_element_type=jnp.float32,
    )
    return ((near_part + far_part).reshape(queries.shape), row_top + jnp.log(row_total))


def spread_back(near_grad, far_grad, flat_index, seq_start, seq_first, total_rows):
    blocks, span, buckets, heads_local, head_size = near_grad.shape
    length_local = blocks * QB
    feature_width = heads_local * head_size
    segment = jnp.zeros((length_local + WIN, buckets, heads_local, head_size), jnp.float32)
    for offset_index in range(WIN // QB + 1):
        piece = near_grad[:, offset_index * QB : (offset_index + 1) * QB].reshape(
            length_local, buckets, heads_local, head_size
        )
        segment = segment.at[offset_index * QB : offset_index * QB + length_local].add(piece)
    full_rows = jnp.zeros((total_rows * buckets * heads_local, head_size), jnp.float32)
    full_rows = full_rows.at[flat_index.reshape(-1)].add(far_grad.reshape(-1, head_size))
    full_rows = full_rows.reshape(total_rows, buckets, feature_width)
    local_part = segment[WIN:].reshape(length_local, buckets, feature_width)
    earlier = jnp.where(seq_first, 0.0, segment[:WIN].reshape(WIN, buckets, feature_width))
    full_rows = lax.dynamic_update_slice_in_dim(
        full_rows,
        lax.dynamic_slice_in_dim(full_rows, seq_start, length_local, 0) + local_part,
        seq_start,
        0,
    )
    earlier_start = jnp.maximum(seq_start - WIN, 0)
    full_rows = lax.dynamic_update_slice_in_dim(
        full_rows,
        lax.dynamic_slice_in_dim(full_rows, earlier_start, WIN, 0) + earlier,
        earlier_start,
        0,
    )
    return full_rows


def attend_back(
    queries, key_rows, value_rows, chosen_now, seq_start, seq_first, log_total, grad_mixed
):
    query_blocks, near_keys, near_values, far_keys, far_values, flat_index, scores = (
        attention_setup(queries, key_rows, value_rows, chosen_now, seq_start, seq_first)
    )
    span = WIN + QB
    score_scale = HDIM ** (-0.5)
    grad_blocks = grad_mixed.reshape(query_blocks.shape)
    weights_full = jnp.exp(scores - log_total)
    softmax_low = weights_full.astype(jnp.bfloat16)
    grad_near_weights = jnp.einsum(
        "bqnhe,btnhe->bnhqt", grad_blocks, near_values, preferred_element_type=jnp.float32
    )
    grad_far_weights = jnp.einsum(
        "bqnhe,nhbke->bnhqk", grad_blocks, far_values, preferred_element_type=jnp.float32
    )
    grad_weights = jnp.concatenate([grad_near_weights, grad_far_weights], -1)
    row_dot = jnp.sum(weights_full * grad_weights, -1, keepdims=True)
    grad_scores = (weights_full * (grad_weights - row_dot)).astype(jnp.bfloat16)
    grad_near, grad_far = (grad_scores[..., :span], grad_scores[..., span:])
    grad_queries = score_scale * (
        jnp.einsum("bnhqt,btnhe->bqnhe", grad_near, near_keys, preferred_element_type=jnp.float32)
        + jnp.einsum("bnhqk,nhbke->bqnhe", grad_far, far_keys, preferred_element_type=jnp.float32)
    )
    near_key_grad = score_scale * jnp.einsum(
        "bnhqt,bqnhe->btnhe", grad_near, query_blocks, preferred_element_type=jnp.float32
    )
    far_key_grad = score_scale * jnp.einsum(
        "bnhqk,bqnhe->nhbke", grad_far, query_blocks, preferred_element_type=jnp.float32
    )
    near_value_grad = jnp.einsum(
        "bnhqt,bqnhe->btnhe",
        softmax_low[..., :span],
        grad_blocks,
        preferred_element_type=jnp.float32,
    )
    far_value_grad = jnp.einsum(
        "bnhqk,bqnhe->nhbke",
        softmax_low[..., span:],
        grad_blocks,
        preferred_element_type=jnp.float32,
    )
    total_rows = key_rows.shape[0]
    key_grad = spread_back(
        near_key_grad, far_key_grad, flat_index, seq_start, seq_first, total_rows
    )
    value_grad = spread_back(
        near_value_grad, far_value_grad, flat_index, seq_start, seq_first, total_rows
    )
    return (grad_queries.reshape(queries.shape), key_grad, value_grad)


def forward_pass(hidden, params, chosen_now, query_mask, seq_start, seq_first, finish):
    (
        ln1_gain,
        ln1_shift,
        w_qkv,
        b_qv,
        w_out,
        b_out,
        ln2_gain,
        ln2_shift,
        w_fc,
        b_fc,
        w_proj,
        b_proj,
    ) = params
    hidden_wide = hidden.astype(jnp.float32)
    normed_all = gather_rows(layer_norm(hidden_wide, ln1_gain, ln1_shift).astype(jnp.bfloat16))
    projected = jnp.einsum("pnd,jdc->jpnc", normed_all, w_qkv, preferred_element_type=jnp.float32)
    queries = (projected[0] + b_qv[0]).astype(jnp.bfloat16)
    key_rows, value_rows = (
        lax.all_gather(projected[1].astype(jnp.bfloat16), "seq", axis=0, tiled=True),
        lax.all_gather((projected[2] + b_qv[1]).astype(jnp.bfloat16), "seq", axis=0, tiled=True),
    )
    attended, log_total = attend(queries, key_rows, value_rows, chosen_now, seq_start, seq_first)
    mixed_rows = (attended * query_mask[:, :, None]).astype(jnp.bfloat16)
    middle = hidden_wide + scatter_product(mixed_rows, w_out, "pnc,cd->pnd") + b_out
    normed_mlp = gather_rows(layer_norm(middle, ln2_gain, ln2_shift).astype(jnp.bfloat16))
    pre_active = (
        jnp.einsum("pnd,df->pnf", normed_mlp, w_fc, preferred_element_type=jnp.float32) + b_fc
    )
    active = gelu_tanh(pre_active).astype(jnp.bfloat16)
    if not finish:
        return (
            normed_all,
            queries,
            key_rows,
            value_rows,
            log_total,
            mixed_rows,
            middle,
            normed_mlp,
            pre_active,
            active,
        )
    output = (middle + scatter_product(active, w_proj, "pnf,fd->pnd") + b_proj).astype(jnp.bfloat16)
    return (output, (key_rows, value_rows))


def backward_pass(hidden, upstream, params, chosen_now, query_mask, seq_start, seq_first):
    (
        ln1_gain,
        ln1_shift,
        w_qkv,
        b_qv,
        w_out,
        b_out,
        ln2_gain,
        ln2_shift,
        w_fc,
        b_fc,
        w_proj,
        b_proj,
    ) = params
    (
        normed_all,
        queries,
        key_rows,
        value_rows,
        log_total,
        mixed_rows,
        middle,
        normed_mlp,
        pre_active,
        active,
    ) = forward_pass(hidden, params, chosen_now, query_mask, seq_start, seq_first, False)
    upstream_all = gather_rows(upstream)
    grad_w_proj = jnp.einsum(
        "pnf,pnd->fd", active, upstream_all, preferred_element_type=jnp.float32
    )
    grad_b_proj = jnp.sum(upstream.astype(jnp.float32), axis=(0, 1))
    grad_active = jnp.einsum(
        "pnd,fd->pnf", upstream_all, w_proj, preferred_element_type=jnp.float32
    )
    unused_value, gelu_pull = jax.vjp(gelu_tanh, pre_active)
    grad_pre = gelu_pull(grad_active)[0].astype(jnp.bfloat16)
    grad_w_fc = jnp.einsum("pnd,pnf->df", normed_mlp, grad_pre, preferred_element_type=jnp.float32)
    grad_b_fc = jnp.sum(grad_pre.astype(jnp.float32), axis=(0, 1))
    grad_normed_mlp = scatter_product(grad_pre, w_fc, "pnf,df->pnd")
    unused_norm, second_pull = jax.vjp(layer_norm, middle, ln2_gain, ln2_shift)
    grad_mid_norm, grad_ln2_gain, grad_ln2_shift = second_pull(grad_normed_mlp)
    grad_middle = upstream.astype(jnp.float32) + grad_mid_norm
    grad_branch = grad_middle.astype(jnp.bfloat16)
    grad_b_out = jnp.sum(grad_branch.astype(jnp.float32), axis=(0, 1))
    branch_all = gather_rows(grad_branch)
    grad_w_out = jnp.einsum(
        "pnc,pnd->cd", mixed_rows, branch_all, preferred_element_type=jnp.float32
    )
    grad_mixed = jnp.einsum(
        "pnd,cd->pnc", branch_all, w_out, preferred_element_type=jnp.float32
    ).astype(jnp.bfloat16) * query_mask[:, :, None].astype(jnp.bfloat16)
    grad_queries, key_grad_all, value_grad_all = attend_back(
        queries, key_rows, value_rows, chosen_now, seq_start, seq_first, log_total, grad_mixed
    )
    key_grad, value_grad = (
        lax.psum_scatter(
            key_grad_all.astype(jnp.bfloat16), "seq", scatter_dimension=0, tiled=True
        ).astype(jnp.float32),
        lax.psum_scatter(
            value_grad_all.astype(jnp.bfloat16), "seq", scatter_dimension=0, tiled=True
        ).astype(jnp.float32),
    )
    grad_project = jnp.stack(
        [
            grad_queries.astype(jnp.bfloat16),
            key_grad.astype(jnp.bfloat16),
            value_grad.astype(jnp.bfloat16),
        ],
        2,
    )
    grad_w_qkv = jnp.einsum(
        "pnd,pnjc->jdc", normed_all, grad_project, preferred_element_type=jnp.float32
    )
    grad_b_qv = jnp.sum(grad_project[:, :, 0::2].astype(jnp.float32), axis=(0, 1))
    grad_normed = scatter_product(grad_project, w_qkv, "pnjc,jdc->pnd")
    unused_first, first_pull = jax.vjp(layer_norm, hidden.astype(jnp.float32), ln1_gain, ln1_shift)
    grad_in_norm, grad_ln1_gain, grad_ln1_shift = first_pull(grad_normed)
    grad_hidden = (grad_middle + grad_in_norm).astype(jnp.bfloat16)
    block_grads = (
        grad_ln1_gain,
        grad_ln1_shift,
        grad_w_qkv,
        grad_b_qv,
        grad_w_out,
        grad_b_out,
        grad_ln2_gain,
        grad_ln2_shift,
        grad_w_fc,
        grad_b_fc,
        grad_w_proj,
        grad_b_proj,
    )
    return (grad_hidden, block_grads)


def on_device(
    inputs,
    cotangent,
    lengths,
    chosen,
    ln1_gain,
    ln1_shift,
    w_qkv,
    b_qv,
    w_out,
    b_out,
    ln2_gain,
    ln2_shift,
    w_fc,
    b_fc,
    w_proj,
    b_proj,
):
    params = tuple(
        (
            weight_array[0]
            for weight_array in (
                ln1_gain,
                ln1_shift,
                w_qkv,
                b_qv,
                w_out,
                b_out,
                ln2_gain,
                ln2_shift,
                w_fc,
                b_fc,
                w_proj,
                b_proj,
            )
        )
    )
    section_index = lax.axis_index("section")
    section_count = lax.axis_size("section")
    seq_index = lax.axis_index("seq")
    tensor_index = lax.axis_index("tensor")
    tensor_count = lax.axis_size("tensor")
    micro_count, rows_local, buckets, feature_width = inputs.shape
    length_local = rows_local * tensor_count
    heads_width = w_qkv.shape[-1]
    seq_start = seq_index * length_local
    seq_first = seq_index == 0
    positions = seq_start + lax.broadcasted_iota(jnp.int32, (micro_count, length_local, buckets), 1)
    mask_all = (positions < lengths[:, None, :]).astype(jnp.float32)
    mask_rows = lax.dynamic_slice_in_dim(mask_all, tensor_index * rows_local, rows_local, 1)
    step_count = micro_count + section_count - 1
    chosen_section = chosen[0]
    received = jnp.zeros((rows_local, buckets, feature_width), jnp.bfloat16)
    stored = jnp.zeros((micro_count, rows_local, buckets, feature_width), jnp.bfloat16)
    outputs = jnp.zeros_like(stored)
    for step_index in range(step_count):
        micro_index = step_index - section_index
        running = (micro_index >= 0) & (micro_index < micro_count)
        slot_index = jnp.clip(micro_index, 0, micro_count - 1)
        block_in = jnp.where(
            section_index == 0, lax.dynamic_index_in_dim(inputs, slot_index, 0, False), received
        )
        chosen_now = lax.dynamic_index_in_dim(chosen_section, slot_index, 0, False)
        query_mask = lax.dynamic_index_in_dim(mask_all, slot_index, 0, False)
        result, key_pair = forward_pass(
            block_in, params, chosen_now, query_mask, seq_start, seq_first, True
        )
        stored = jnp.where(
            running, lax.dynamic_update_index_in_dim(stored, block_in, slot_index, 0), stored
        )
        outputs = jnp.where(
            running, lax.dynamic_update_index_in_dim(outputs, result, slot_index, 0), outputs
        )
        received = from_behind(result, "section", 1)
    back_received = jnp.zeros((rows_local, buckets, feature_width), jnp.bfloat16)
    in_grads = jnp.zeros_like(stored)
    totals = None
    for step_index in range(step_count):
        micro_index = step_index - (section_count - 1 - section_index)
        running = (micro_index >= 0) & (micro_index < micro_count)
        slot_index = jnp.clip(micro_index, 0, micro_count - 1)
        chosen_now = lax.dynamic_index_in_dim(chosen_section, slot_index, 0, False)
        query_mask = lax.dynamic_index_in_dim(mask_all, slot_index, 0, False)
        local_mask = lax.dynamic_index_in_dim(mask_rows, slot_index, 0, False)
        top_grad = (
            lax.dynamic_index_in_dim(cotangent, slot_index, 0, False).astype(jnp.float32)
            * local_mask[:, :, None]
        ).astype(jnp.bfloat16)
        upstream = jnp.where(section_index == section_count - 1, top_grad, back_received)
        hidden = lax.dynamic_index_in_dim(stored, slot_index, 0, False)
        grad_hidden, block_grads = backward_pass(
            hidden, upstream, params, chosen_now, query_mask, seq_start, seq_first
        )
        block_grads = tuple(
            (jnp.where(running, grad_part, jnp.zeros_like(grad_part)) for grad_part in block_grads)
        )
        totals = (
            block_grads
            if step_index == 0
            else tuple(
                (total_part + grad_part for total_part, grad_part in zip(totals, block_grads))
            )
        )
        in_grads = jnp.where(
            running, lax.dynamic_update_index_in_dim(in_grads, grad_hidden, slot_index, 0), in_grads
        )
        back_received = from_behind(grad_hidden, "section", -1)
    (
        sum_ln1_gain,
        sum_ln1_shift,
        sum_w_qkv,
        sum_b_qv,
        sum_w_out,
        sum_b_out,
        sum_ln2_gain,
        sum_ln2_shift,
        sum_w_fc,
        sum_b_fc,
        sum_w_proj,
        sum_b_proj,
    ) = totals
    part_qkv, part_out, part_fc, part_proj = (
        lax.psum_scatter(
            sum_w_qkv.astype(jnp.bfloat16), "seq", scatter_dimension=1, tiled=True
        ).astype(jnp.float32),
        lax.psum_scatter(
            sum_w_out.astype(jnp.bfloat16), "seq", scatter_dimension=1, tiled=True
        ).astype(jnp.float32),
        lax.psum_scatter(
            sum_w_fc.astype(jnp.bfloat16), "seq", scatter_dimension=0, tiled=True
        ).astype(jnp.float32),
        lax.psum_scatter(
            sum_w_proj.astype(jnp.bfloat16), "seq", scatter_dimension=1, tiled=True
        ).astype(jnp.float32),
    )
    bias_qv = lax.dynamic_update_slice_in_dim(
        jnp.zeros((2, feature_width), jnp.float32), sum_b_qv, tensor_index * heads_width, 1
    )
    units_local = sum_b_fc.shape[0]
    bias_fc = lax.dynamic_update_slice_in_dim(
        jnp.zeros((units_local * tensor_count,), jnp.float32),
        sum_b_fc,
        tensor_index * units_local,
        0,
    )
    small_sums = lax.psum(
        (
            sum_ln1_gain,
            sum_ln1_shift,
            bias_qv,
            sum_b_out,
            sum_ln2_gain,
            sum_ln2_shift,
            bias_fc,
            sum_b_proj,
        ),
        ("seq", "tensor"),
    )
    return (
        outputs[None],
        in_grads[None],
        small_sums[0][None],
        small_sums[1][None],
        part_qkv[None],
        small_sums[2][None],
        part_out[None],
        small_sums[3][None],
        small_sums[4][None],
        small_sums[5][None],
        part_fc[None],
        small_sums[6][None],
        part_proj[None],
        small_sums[7][None],
    )


STREAMS = 2
NRM, NMLP, UPS, BRN, ACT, GPRE, MIX, DQKV = range(8)
F32 = jnp.float32
LOW = jnp.bfloat16
MESH_ID = pl.DeviceIdType.MESH


def dot_nn(left, right):
    return lax.dot_general(left, right, (((1,), (0,)), ((), ())), preferred_element_type=F32)


def dot_nt(left, right):
    return lax.dot_general(left, right, (((1,), (1,)), ((), ())), preferred_element_type=F32)


def dot_tn(left, right):
    return lax.dot_general(left, right, (((0,), (0,)), ((), ())), preferred_element_type=F32)


def standard(rows):
    centred = rows - jnp.mean(rows, axis=-1, keepdims=True)
    scale = lax.rsqrt(jnp.mean(centred * centred, axis=-1, keepdims=True) + NORM_EPS)
    return centred * scale, scale


def standard_back(grad, xhat, scale):
    inner = jnp.mean(grad * xhat, axis=-1, keepdims=True)
    return scale * (grad - jnp.mean(grad, axis=-1, keepdims=True) - xhat * inner)


def column_sum(rows):
    return jnp.sum(rows.astype(F32), axis=0, keepdims=True)


def relay_kernel(names, *refs):
    r = types.SimpleNamespace(**dict(zip(names, refs)))
    a, c, t = (lax.axis_index(name) for name in ("section", "seq", "tensor"))
    lines = lax.axis_size("section")
    chips = lax.axis_size("tensor")
    rows, buckets, width = r.inputs.shape[1:]
    half_width = width // 2
    local = rows * chips
    total = 2 * local
    stream_rows = local // STREAMS
    head_width = r.wo_in.shape[0]
    heads = head_width // HDIM
    blocks = local // QB
    units = r.wp_in.shape[0]
    scale = HDIM ** (-0.5)
    streams = range(STREAMS)

    def remote(src, dst, send, recv, **target):
        return pltpu.make_async_remote_copy(
            src_ref=src,
            dst_ref=dst,
            send_sem=send,
            recv_sem=recv,
            device_id=target,
            device_id_type=MESH_ID,
        )

    def drain(ref, sem):
        pltpu.make_async_copy(ref, ref, sem).wait()

    def row_block(index, size):
        return pl.ds(pl.multiple_of(index * size, size), size)

    near_chip = t + 1 - 2 * (t % 2)
    over_chip = (t + 2) % 4
    across_chip = 3 - t
    middle_chip = (t == 1) | (t == 2)
    end_chip = (t == 0) | (t == 3)
    owned = stream_rows // 2
    mine = row_block(t - 1, owned)
    my_half = row_block(c, local)

    r.kv[...] = jnp.zeros(r.kv.shape, LOW)

    barrier = pltpu.get_barrier_semaphore()
    greeted = 0
    for line in range(lines):
        for chip in range(chips):
            for core in range(2):
                if (line, chip, core) != (0, 0, 0) and (core == 0 or line * chip == 0):
                    there = {
                        "section": (a + line) % lines,
                        "seq": (c + core) % 2,
                        "tensor": (t + chip) % chips,
                    }
                    pl.semaphore_signal(barrier, inc=1, device_id=there, device_id_type=MESH_ID)
                    greeted += 1
    pl.semaphore_wait(barrier, greeted)

    def beside(s):
        return s + 1 - 2 * (s % 2)

    def above(s):
        return (s + 2) % 4

    def store(p):
        return (r.wq, r.wo, r.wf, r.wp)[p]

    def source(p):
        return (r.wq_in, r.wo_in, r.wf_in, r.wp_in)[p]

    def height(p):
        return source(p).shape[0]

    def core_half(p, s, core):
        return store(p).at[s, row_block(core, height(p) // 2)]

    def first_hop(p, s, neighbour, which):
        return remote(
            source(p).at[row_block(c, height(p) // 2)],
            core_half(p, s, c),
            r.w_first_s.at[p, which],
            r.w_first_r.at[s, p],
            section=neighbour,
        )

    def second_hop(p, s, which):
        view = store(p).at[s, row_block(2 * c + which, height(p) // 4)]
        return remote(
            view, view, r.w_second_s.at[s, p], r.w_second_r.at[s, p, which], section=3 - s
        )

    def core_hop(p, s, core):
        view = core_half(p, s, core)
        return remote(view, view, r.w_core_s.at[s, p], r.w_core_r.at[s, p], seq=1 - c)

    def own_copy(p):
        return pltpu.make_async_copy(source(p), store(p).at[a], r.w_own.at[p])

    def pass_on(s, p, which):
        line = (beside(s), above(s))[which]

        @pl.when(a == line)
        def _():
            first_hop(p, s, line, which).wait_recv()
            second_hop(p, s, which).start()
            core_hop(p, s, c).start()

    def pass_all(s, pieces):
        for p in pieces:
            for which in range(2):
                pass_on(s, p, which)

    def pass_far(s, p):
        @pl.when(a == 3 - s)
        def _():
            second_hop(p, s, 0).wait_recv()
            second_hop(p, s, 1).wait_recv()
            core_hop(p, s, c).start()

    def need(s, p):
        @pl.when(s == 0)
        def _():
            if p < 2:
                pass_all(0, (p,))
            pass_far(0, p)

        @pl.when(a == s)
        def _():
            own_copy(p).wait()

        @pl.when(a != s)
        def _():
            core_hop(p, s, 1 - c).wait_recv()

    def small_copy(step, line, slot):
        return remote(
            r.small_own, r.small.at[slot], r.small_s.at[step], r.small_r.at[slot], section=line
        )

    def count_copy(step, line, slot):
        return remote(
            r.count_own.at[line],
            r.count.at[slot],
            r.count_s.at[step],
            r.count_r.at[slot],
            section=line,
        )

    singles = (r.ln1_gain, r.ln1_shift, r.ln2_gain, r.ln2_shift, r.b_out, r.b_proj)
    for place, single in enumerate(singles):
        r.small_own[place : place + 1] = single[...]
    r.small_own[6:7, :units] = r.b_fc[...]
    r.small_own[7:8, :head_width] = r.b_qv[0:1]
    r.small_own[7:8, half_width : half_width + head_width] = r.b_qv[1:2]
    for step in range(1, lines):
        small_copy(step - 1, (a + step) % lines, a).start()
    for p in range(4):
        for which, line in enumerate((beside(a), above(a))):
            first_hop(p, a, line, which).start()
    for p in range(4):
        own_copy(p).start()
    r.small[a] = r.small_own[...]

    def iota(shape, dimension):
        return lax.broadcasted_iota(jnp.int32, shape, dimension)

    square = jnp.where(iota((KSEL, KSEL), 0) == iota((KSEL, KSEL), 1), 1.0, 0.0).astype(LOW)
    position = iota((KSEL, total), 1).astype(F32)
    for pair in range(lines * heads):
        line, head = pair // heads, pair % heads
        columns = dot_nt(square, r.chosen[pair].astype(F32).astype(LOW))
        for block in range(blocks):
            pick = head * blocks + block
            r.count_own[line, pick : pick + 1, :] = jnp.sum(
                jnp.where(columns[:, block : block + 1] == position, 1.0, 0.0),
                axis=0,
                keepdims=True,
            )
    for step in range(1, lines):
        count_copy(step - 1, (a + step) % lines, a).start()
    r.count[a] = r.count_own[a]

    NEAR, OVER, ACROSS = range(3)

    def gather(buffer, s, kind, j, owner, target, slot):
        view = buffer.at[s, j, row_block(owner - 1, owned)]
        return remote(
            view, view, r.ag_s.at[kind, j, slot], r.ag_r.at[kind, j, slot], tensor=target
        )

    def used_before(s, kind):
        return s > 0 if kind < 2 else s < lines - 1

    def gather_start(buffer, s, kind, j):
        @pl.when(used_before(s, kind))
        def _():
            gather_sent(buffer, s, kind, j)

        gather(buffer, s, kind, j, t, over_chip, OVER).start()
        gather(buffer, s, kind, j, t, across_chip, ACROSS).start()
        gather(buffer, s, kind, j, t, near_chip, NEAR).start()

    def gather_wait(buffer, s, kind, j):
        @pl.when(middle_chip)
        def _():
            gather(buffer, s, kind, j, across_chip, across_chip, ACROSS).wait_recv()

        @pl.when(end_chip)
        def _():
            gather(buffer, s, kind, j, near_chip, near_chip, NEAR).wait_recv()
            gather(buffer, s, kind, j, over_chip, over_chip, OVER).wait_recv()

    def gather_sent(buffer, s, kind, j):
        gather(buffer, s, kind, j, t, over_chip, OVER).wait_send()
        gather(buffer, s, kind, j, t, across_chip, ACROSS).wait_send()
        gather(buffer, s, kind, j, t, near_chip, NEAR).wait_send()

    def scatter(s, kind, j, owner, slot):
        return remote(
            r.part.at[kind, j, row_block(owner - 1, owned)],
            r.arrived.at[s, kind, j, slot],
            r.rs_s.at[kind, j, slot],
            r.rs_r.at[kind, j, slot],
            tensor=owner,
        )

    def scatter_start(s, kind, j, product):
        @pl.when(used_before(s, kind))
        def _():
            scatter_sent(s, kind, j)

        r.part[kind, j] = product.astype(LOW)

        @pl.when(end_chip)
        def _():
            scatter(s, kind, j, over_chip, OVER).start()
            scatter(s, kind, j, near_chip, NEAR).start()

        @pl.when(middle_chip)
        def _():
            scatter(s, kind, j, across_chip, ACROSS).start()

    def scatter_sum(s, kind, j):
        result = r.part[kind, j, mine].astype(F32)
        for slot in (NEAR, ACROSS, OVER):
            scatter(s, kind, j, t, slot).wait_recv()
            result = result + r.arrived[s, kind, j, slot].astype(F32)
        return result

    def scatter_sent(s, kind, j):
        @pl.when(end_chip)
        def _():
            scatter(s, kind, j, over_chip, OVER).wait_send()
            scatter(s, kind, j, near_chip, NEAR).wait_send()

        @pl.when(middle_chip)
        def _():
            scatter(s, kind, j, across_chip, ACROSS).wait_send()

    own_rows = (r.nrm, r.nmlp, r.ups, r.brn, r.act, r.gpre, r.mix, r.dqkv)
    all_rows = (
        r.all_nrm,
        r.all_nmlp,
        r.all_ups,
        r.all_brn,
        r.all_act,
        r.all_gpre,
        r.all_mix,
        r.all_dqkv,
    )

    def rows_copy(index, s, same, stays=False):
        core = c if same else 1 - c
        src = own_rows[index].at[s]
        dst = all_rows[index].at[a, c]
        if index <= BRN:
            src = src.at[:, :, row_block(core, half_width)]
        recv = r.rows_r.at[index]
        if stays:
            return pltpu.make_async_copy(src, dst, recv)
        if same:
            return remote(src, dst, r.rows_s.at[index, s, 0], recv, section=s)
        return remote(src, dst, r.rows_s.at[index, s, 1], recv, section=s, seq=1 - c)

    def rows_start(index, s):
        @pl.when(a == s)
        def _():
            rows_copy(index, s, True, True).start()

        @pl.when(a != s)
        def _():
            rows_copy(index, s, True).start()

        if index <= BRN:
            rows_copy(index, s, False).start()

    def forward_rows(s):
        for index in (NRM, MIX, NMLP, ACT):
            rows_start(index, s)

    def rows_sent(index, s):
        @pl.when(a != s)
        def _():
            rows_copy(index, s, True).wait_send()

        if index <= BRN:
            rows_copy(index, s, False).wait_send()

    def share_copy(index, core):
        view = all_rows[index].at[:, core]
        return remote(view, view, r.share_s.at[index - ACT], r.share_r.at[index - ACT], seq=1 - c)

    def share(index):
        drain(all_rows[index].at[:, c], r.rows_r.at[index])
        share_copy(index, c).start()

    def norm_copy(s):
        return remote(
            r.norm_part.at[s], r.norm_all.at[a], r.norm_s.at[s], r.norm_r, section=s
        )

    def norm_start(s):
        @pl.when(a == s)
        def _():
            pltpu.make_async_copy(r.norm_part.at[s], r.norm_all.at[a], r.norm_r).start()

        @pl.when(a != s)
        def _():
            norm_copy(s).start()

    def home_copy(what, s, j):
        src, dst, send, recv = what
        chip = 2 * j + t - 1
        return remote(src.at[s, j], dst.at[a], send.at[s, j], recv, section=s, tensor=chip)

    def home_start(what, s):
        @pl.when(middle_chip)
        def _():
            for j in streams:
                home_copy(what, s, j).start()

    def home_sent(what, s):
        @pl.when(middle_chip)
        def _():
            for j in streams:
                home_copy(what, s, j).wait_send()

    out_home = (r.out_low, r.acts, r.out_s, r.out_r)
    grad_home = (r.grad_low, r.grads, r.grad_s, r.grad_r)

    length = r.lengths[a // buckets, a % buckets]
    key = iota((stream_rows, total), 1)
    for j in streams:
        query = c * local + j * stream_rows + iota((stream_rows, total), 0)
        r.near[j] = jnp.where((query >= key) & (query - key < WIN), 1.0, 0.0)
    key_row = iota((1, total), 1)

    def row_mask(place):
        return jnp.where(place < length, 1.0, 0.0)

    def stream_mask(j):
        return row_mask(c * local + j * stream_rows + iota((stream_rows, 1), 0))

    def multiplicity(s, j, head):
        block = j * stream_rows // QB
        pick = head * blocks + block
        limit = (c * blocks + block) * QB - WIN
        return r.near[j] + jnp.where(key_row <= limit, r.count[s, pick : pick + 1, :], 0.0)

    def head_cols(head):
        return slice(head * HDIM, (head + 1) * HDIM)

    def kv_copy(s, j):
        view = r.kv.at[s, :, j * stream_rows : (j + 1) * stream_rows]
        return remote(view, view, r.kv_s.at[s, j], r.kv_r.at[s, j], seq=1 - c)

    def dkv_copy(s):
        return remote(r.dkv_out.at[s], r.dkv_in.at[s], r.dkv_s.at[s], r.dkv_r.at[s], seq=1 - c)

    def own_sequence(ref):
        both = ref[a // buckets].astype(F32)
        picked = both[:, 0, :]
        for bucket in range(1, buckets):
            picked = jnp.where(a % buckets == bucket, both[:, bucket, :], picked)
        return picked

    def first_copy(stream):
        return remote(
            r.first_out, r.first_in.at[stream], r.first_s, r.first_r.at[stream], tensor=1 + t % 2
        )

    own_place = c * local + t * rows + iota((rows, 1), 0)
    r.first_out[0] = own_sequence(r.inputs).astype(LOW)
    r.first_out[1] = (own_sequence(r.cotangent) * row_mask(own_place)).astype(LOW)
    first_copy(t // 2).start()
    r.norm_part[...] = jnp.zeros_like(r.norm_part)

    def first_rows(j):
        @pl.when(middle_chip)
        def _():
            first_copy(j).wait_recv()
            r.hidden[j] = r.first_in[j, 0].astype(F32)
            r.upstream[j] = r.first_in[j, 1]

    def on_owner(stage):
        def run(s, j):
            @pl.when(middle_chip)
            def _():
                stage(s, j)

        return run

    @on_owner
    def enter(s, j):
        xhat, inverse = standard(r.hidden[j])
        r.xhat1[s, j] = xhat
        r.inv1[s, j] = jnp.broadcast_to(inverse, (owned, 128))
        r.nrm[s, j, mine] = (xhat * r.small[s, 0:1] + r.small[s, 1:2]).astype(LOW)
        gather_start(r.nrm, s, 0, j)

    def project(s, j):
        gather_wait(r.nrm, s, 0, j)
        normed = r.nrm[s, j]
        place = row_block(c * STREAMS + j, stream_rows)
        bias_v = r.small[s, 7:8, half_width : half_width + head_width]
        key_rows = dot_nt(normed, r.wq[s, head_width : 2 * head_width])
        value_rows = dot_nt(normed, r.wq[s, 2 * head_width : 3 * head_width]) + bias_v
        r.kv[s, 0, place] = key_rows.astype(LOW)
        r.kv[s, 1, place] = value_rows.astype(LOW)

    def ask(s, j):
        queries = dot_nt(r.nrm[s, j], r.wq[s, 0:head_width]) + r.small[s, 7:8, :head_width]
        r.qry[s, j] = queries.astype(LOW)

    def attend_line(s, j):
        mixed = []
        for head in range(heads):
            cols = head_cols(head)
            times = multiplicity(s, j, head)
            scores = scale * dot_nt(r.qry[s, j, :, cols], r.kv[s, 0, :, cols])
            scores = jnp.where(times > 0.0, scores, MASKED)
            top = jnp.max(scores, axis=-1, keepdims=True)
            terms = times * jnp.exp(scores - top)
            weights = terms / jnp.sum(terms, axis=-1, keepdims=True)
            r.soft[s, j, head] = weights
            mixed.append(dot_nn(weights.astype(LOW), r.kv[s, 1, :, cols]))
        r.mix[s, j] = (jnp.concatenate(mixed, axis=-1) * stream_mask(j)).astype(LOW)

    def leave_attention(s, j):
        scatter_start(s, 0, j, dot_nn(r.mix[s, j], r.wo[s]))

    @on_owner
    def between(s, j):
        middle = r.hidden[j] + scatter_sum(s, 0, j) + r.small[s, 4:5]
        r.middle[j] = middle
        xhat, inverse = standard(middle)
        r.xhat2[s, j] = xhat
        r.inv2[s, j] = jnp.broadcast_to(inverse, (owned, 128))
        r.nmlp[s, j, mine] = (xhat * r.small[s, 2:3] + r.small[s, 3:4]).astype(LOW)
        gather_start(r.nmlp, s, 1, j)

    def feed(s, j):
        gather_wait(r.nmlp, s, 1, j)
        before = dot_nn(r.nmlp[s, j], r.wf[s]) + r.small[s, 6:7, :units]
        bend = jnp.tanh(0.7978845608028654 * (before + 0.044715 * before * before * before))
        r.act[s, j] = (0.5 * before * (1.0 + bend)).astype(LOW)
        r.slope[s, j] = 0.5 * (1.0 + bend) + 0.5 * before * (1.0 - bend * bend) * (
            0.7978845608028654 * (1.0 + 3 * 0.044715 * before * before)
        )


    def leave_feed(s, j):
        scatter_start(s, 1, j, dot_nn(r.act[s, j], r.wp[s]))

    @on_owner
    def finish(s, j):
        result = r.middle[j] + scatter_sum(s, 1, j) + r.small[s, 5:6]
        r.out_low[s, j] = result.astype(LOW)
        r.hidden[j] = result.astype(LOW).astype(F32)

    def small_ready(s):
        @pl.when(a != s)
        def _():
            small_copy(0, a, s).wait_recv()

    small_ready(0)
    for j in streams:
        first_rows(j)
        enter(0, j)

    def forward(s, _):
        need(s, 0)
        need(s, 1)

        @pl.when(a != s)
        def _():
            count_copy(0, a, s).wait_recv()

        for j in streams:
            project(s, j)

            @pl.when(c == 0)
            def _():
                kv_copy(s, j).start()

            ask(s, j)
            if j == 0:

                @pl.when(c == 1)
                def _():
                    for other in streams:
                        kv_copy(s, other).wait_recv()

            attend_line(s, j)
            leave_attention(s, j)

        @pl.when(s == 0)
        def _():
            pass_all(0, (2,))
            for later in range(1, lines):
                pass_all(later, (0, 1, 2))

        @pl.when(s == 1)
        def _():
            pass_far(1, 2)
            pass_far(1, 3)
            for later in range(2, lines):
                for p in range(4):
                    pass_far(later, p)

        for j in streams:
            between(s, j)
        @pl.when(s == 0)
        def _():
            for later in range(lines):
                pass_all(later, (3,))

        need(s, 2)
        for j in streams:
            feed(s, j)
            if j == 0:
                need(s, 3)
            leave_feed(s, j)


        @pl.when(s >= 2)
        def _():
            forward_rows(s - 2)


        @pl.when(s + 1 < lines)
        def _():
            small_ready(s + 1)

        for j in streams:
            finish(s, j)

            @pl.when(s + 1 < lines)
            def _():
                enter(s + 1, j)

        home_start(out_home, s)

        @pl.when(s == 0)
        def _():
            pass_far(1, 0)
            pass_far(1, 1)

        return 0

    lax.fori_loop(0, lines, forward, 0)

    @on_owner
    def turn(s, j):
        upstream = r.upstream[j]
        r.ups[s, j, mine] = upstream
        gather_start(r.ups, s, 2, j)
        r.norm_part[s, 5:6] += column_sum(upstream)

    def feed_back(s, j):
        gather_wait(r.ups, s, 2, j)
        grad_pre = (dot_nt(r.ups[s, j], r.wp[s]) * r.slope[s, j]).astype(LOW)
        r.gpre[s, j] = grad_pre
        scatter_start(s, 2, j, dot_nt(grad_pre, r.wf[s]))
        r.norm_part[s, 6:7, :units] += column_sum(grad_pre)

    @on_owner
    def between_back(s, j):
        grad = scatter_sum(s, 2, j)
        xhat = r.xhat2[s, j]
        upstream = r.upstream[j].astype(F32)
        grad_middle = upstream + standard_back(
            grad * r.small[s, 2:3], xhat, r.inv2[s, j, :, 0:1]
        )
        r.middle[j] = grad_middle
        branch = grad_middle.astype(LOW)
        r.brn[s, j, mine] = branch
        gather_start(r.brn, s, 3, j)
        r.norm_part[s, 2:3] += column_sum(grad * xhat)
        r.norm_part[s, 3:4] += column_sum(grad)
        r.norm_part[s, 4:5] += column_sum(branch)

    def mixed_back(s, j):
        gather_wait(r.brn, s, 3, j)
        r.gmix[j] = (dot_nt(r.brn[s, j], r.wo[s]) * stream_mask(j)).astype(LOW)

    def attend_line_back(s, j):
        grad_q, grad_k, grad_v = [], [], []
        for head in range(heads):
            cols = head_cols(head)
            weights = r.soft[s, j, head]
            grad_head = r.gmix[j, :, cols]
            grad_weights = dot_nt(grad_head, r.kv[s, 1, :, cols])
            inner = jnp.sum(weights * grad_weights, axis=-1, keepdims=True)
            grad_scores = (weights * (grad_weights - inner)).astype(LOW)
            grad_k.append(scale * dot_tn(grad_scores, r.qry[s, j, :, cols]))
            grad_v.append(dot_tn(weights.astype(LOW), grad_head))
            grad_q.append(scale * dot_nn(grad_scores, r.kv[s, 0, :, cols]))
        for which, grad in enumerate((grad_k, grad_v)):
            grad = jnp.concatenate(grad, axis=-1)
            r.dkv_all[which] = grad if j == STREAMS - 1 else r.dkv_all[which] + grad
        grad_q = jnp.concatenate(grad_q, axis=-1).astype(LOW)
        r.dqkv[s, 0, j] = grad_q
        r.norm_part[s, 7:8, :head_width] += column_sum(grad_q)

    def join_keys(s, j):
        for which in range(2):
            joined = r.dkv_all[which, row_block(c * STREAMS + j, stream_rows)].astype(LOW)
            r.dqkv[s, 1 + which, j] = joined
            if which == 1:
                lanes = slice(half_width, half_width + head_width)
                r.norm_part[s, 7:8, lanes] += column_sum(joined)

    def leave_back(s, j):
        product = dot_nn(r.dqkv[s, 0, j], r.wq[s, 0:head_width])
        for which in range(1, 3):
            weight = r.wq[s, which * head_width : (which + 1) * head_width]
            product = product + dot_nn(r.dqkv[s, which, j], weight)
        scatter_start(s, 3, j, product)

    @on_owner
    def finish_back(s, j):
        grad = scatter_sum(s, 3, j)
        xhat = r.xhat1[s, j]
        result = r.middle[j] + standard_back(
            grad * r.small[s, 0:1], xhat, r.inv1[s, j, :, 0:1]
        )
        r.upstream[j] = result.astype(LOW)
        r.grad_low[s, j] = result.astype(LOW)
        r.norm_part[s, 0:1] += column_sum(grad * xhat)
        r.norm_part[s, 1:2] += column_sum(grad)

    last_first = tuple(reversed(streams))
    for j in last_first:
        turn(lines - 1, j)

    def backward(index, _):
        s = lines - 1 - index
        for j in last_first:
            feed_back(s, j)
        rows_start(UPS, s)
        rows_start(GPRE, s)

        @pl.when(index < 2)
        def _():
            forward_rows(lines - 2 + index)

        @pl.when(index == lines - 1)
        def _():
            share(ACT)
            share(MIX)

        for j in last_first:
            between_back(s, j)
        for j in last_first:
            mixed_back(s, j)
            attend_line_back(s, j)

            @pl.when(c == 1)
            def _():
                join_keys(s, j)
                leave_back(s, j)

        rows_start(BRN, s)

        @pl.when(c == 1)
        def _():
            r.dkv_out[s] = r.dkv_all[:, 0:local].astype(LOW)
            dkv_copy(s).start()

        @pl.when(c == 0)
        def _():
            dkv_copy(s).wait_recv()
            r.dkv_all[:, 0:local] += r.dkv_in[s].astype(F32)
            for j in last_first:
                join_keys(s, j)
                leave_back(s, j)

        rows_start(DQKV, s)
        for j in last_first:
            finish_back(s, j)

            @pl.when(s > 0)
            def _():
                turn(s - 1, j)

        norm_start(s)
        home_start(grad_home, s)
        return 0

    lax.fori_loop(0, lines, backward, 0)

    share(GPRE)
    share(DQKV)

    drain(r.norm_all, r.norm_r)
    slot = c * chips + t
    norm_sum = r.norm_all[0]
    for line in range(1, lines):
        norm_sum = norm_sum + r.norm_all[line]
    r.ends[slot] = norm_sum

    def ends_copy(step):
        core, chip = step // chips, step % chips
        view = r.ends.at[slot]
        return remote(
            view,
            view,
            r.ends_s.at[step - 1],
            r.ends_r,
            seq=(c + core) % 2,
            tensor=(t + chip) % chips,
        )

    for step in range(1, 2 * chips):
        ends_copy(step).start()

    for kind, buffer in enumerate((r.nrm, r.nmlp, r.ups, r.brn)):
        for j in streams:
            scatter_sent(0, kind, j)

            @pl.when(middle_chip)
            def _():
                gather_sent(buffer, 0, kind, j)

    for index in range(ACT):
        drain(all_rows[index], r.rows_r.at[index])
    for index in range(ACT, 8):
        share_copy(index, 1 - c).wait_recv()
        share_copy(index, c).wait_send()
    drain(r.acts, r.out_r)
    drain(r.grads, r.grad_r)
    drain(r.ends.at[0 : 2 * chips - 1], r.ends_r)
    for step in range(1, 2 * chips):
        ends_copy(step).wait_send()
    for step in range(1, lines):
        small_copy(step - 1, (a + step) % lines, a).wait_send()
        count_copy(step - 1, (a + step) % lines, a).wait_send()
    for p in range(4):
        for which, line in enumerate((beside(a), above(a))):
            first_hop(p, a, line, which).wait_send()

    first_copy(t // 2).wait_send()

    def sent(s, _):
        home_sent(out_home, s)
        home_sent(grad_home, s)

        @pl.when(a != s)
        def _():
            norm_copy(s).wait_send()

        @pl.when(c == 0)
        def _():
            for j in streams:
                kv_copy(s, j).wait_send()

        @pl.when(c == 1)
        def _():
            dkv_copy(s).wait_send()

        for index in range(8):
            rows_sent(index, s)
        for p in range(4):

            @pl.when((a == beside(s)) | (a == above(s)))
            def _():
                second_hop(p, s, 0).wait_send()

            @pl.when(a != s)
            def _():
                core_hop(p, s, c).wait_send()

        return 0

    lax.fori_loop(0, lines, sent, 0)


def relay_call(inputs, cotangent, lengths, chosen, singles, weights):
    lines = lax.axis_size("section")
    chips = lax.axis_size("tensor")
    rows, buckets, width = inputs.shape[1:]
    local, total, half = rows * chips, 2 * rows * chips, width // 2
    head_width, units = weights["wo_in"].shape[0], weights["wp_in"].shape[0]
    heads = head_width // HDIM
    stream = local // STREAMS
    peers, owned = chips - 1, stream // 2
    vmem, dma = pltpu.VMEM, pltpu.SemaphoreType.DMA
    operands = dict(
        inputs=inputs,
        cotangent=cotangent,
        lengths=lengths,
        chosen=chosen,
        **singles,
        **weights,
    )

    def space(name):
        if name in weights:
            return pl.ANY
        return pltpu.SMEM if operands[name] is lengths else pltpu.VMEM

    sums = dict(
        acts=((lines, rows, width), LOW),
        grads=((lines, rows, width), LOW),
        ends=((2 * chips, 8, width), F32),
    )
    gathered = dict(
        all_nrm=((lines, 2, STREAMS, stream, half), LOW),
        all_nmlp=((lines, 2, STREAMS, stream, half), LOW),
        all_ups=((lines, 2, STREAMS, stream, half), LOW),
        all_brn=((lines, 2, STREAMS, stream, half), LOW),
        all_act=((lines, 2, STREAMS, stream, units), LOW),
        all_gpre=((lines, 2, STREAMS, stream, units), LOW),
        all_mix=((lines, 2, STREAMS, stream, head_width), LOW),
        all_dqkv=((lines, 2, 3, STREAMS, stream, head_width), LOW),
    )
    outputs = dict(**sums, **gathered)
    scratch = dict(
        wq=vmem((lines,) + weights["wq_in"].shape, LOW),
        wo=vmem((lines,) + weights["wo_in"].shape, LOW),
        wf=vmem((lines,) + weights["wf_in"].shape, LOW),
        wp=vmem((lines,) + weights["wp_in"].shape, LOW),
        small_own=vmem((8, width), F32),
        small=vmem((lines, 8, width), F32),
        count_own=vmem((lines, 8, total), F32),
        count=vmem((lines, 8, total), F32),
        hidden=vmem((STREAMS, owned, width), F32),
        middle=vmem((STREAMS, owned, width), F32),
        upstream=vmem((STREAMS, owned, width), LOW),
        first_out=vmem((2, owned, width), LOW),
        first_in=vmem((STREAMS, 2, owned, width), LOW),
        xhat1=vmem((lines, STREAMS, owned, width), F32),
        inv1=vmem((lines, STREAMS, owned, 128), F32),
        xhat2=vmem((lines, STREAMS, owned, width), F32),
        inv2=vmem((lines, STREAMS, owned, 128), F32),
        nrm=vmem((lines, STREAMS, stream, width), LOW),
        nmlp=vmem((lines, STREAMS, stream, width), LOW),
        ups=vmem((lines, STREAMS, stream, width), LOW),
        brn=vmem((lines, STREAMS, stream, width), LOW),
        act=vmem((lines, STREAMS, stream, units), LOW),
        gpre=vmem((lines, STREAMS, stream, units), LOW),
        slope=vmem((lines, STREAMS, stream, units), F32),
        mix=vmem((lines, STREAMS, stream, head_width), LOW),
        qry=vmem((lines, STREAMS, stream, head_width), LOW),
        gmix=vmem((STREAMS, stream, head_width), LOW),
        dqkv=vmem((lines, 3, STREAMS, stream, head_width), LOW),
        kv=vmem((lines, 2, total, head_width), LOW),
        soft=vmem((lines, STREAMS, heads, stream, total), F32),
        near=vmem((STREAMS, stream, total), F32),
        dkv_all=vmem((2, total, head_width), F32),
        dkv_out=vmem((lines, 2, local, head_width), LOW),
        dkv_in=vmem((lines, 2, local, head_width), LOW),
        part=vmem((4, STREAMS, stream, width), LOW),
        arrived=vmem((lines, 4, STREAMS, peers, owned, width), LOW),
        out_low=vmem((lines, STREAMS, owned, width), LOW),
        grad_low=vmem((lines, STREAMS, owned, width), LOW),
        norm_part=vmem((lines, 8, width), F32),
        norm_all=vmem((lines, 8, width), F32),
        w_first_s=dma((4, 2)),
        w_first_r=dma((lines, 4)),
        w_second_s=dma((lines, 4)),
        w_second_r=dma((lines, 4, 2)),
        w_core_s=dma((lines, 4)),
        w_core_r=dma((lines, 4)),
        w_own=dma((4,)),
        small_s=dma((lines - 1,)),
        small_r=dma((lines,)),
        count_s=dma((lines - 1,)),
        count_r=dma((lines,)),
        ag_s=dma((4, STREAMS, peers)),
        ag_r=dma((4, STREAMS, peers)),
        rs_s=dma((4, STREAMS, peers)),
        rs_r=dma((4, STREAMS, peers)),
        kv_s=dma((lines, STREAMS)),
        kv_r=dma((lines, STREAMS)),
        dkv_s=dma((lines,)),
        dkv_r=dma((lines,)),
        rows_s=dma((8, lines, 2)),
        rows_r=dma((8,)),
        share_s=dma((4,)),
        share_r=dma((4,)),
        first_s=dma,
        first_r=dma((STREAMS,)),
        out_s=dma((lines, STREAMS)),
        out_r=dma,
        grad_s=dma((lines, STREAMS)),
        grad_r=dma,
        norm_s=dma((lines,)),
        norm_r=dma,
        ends_s=dma((2 * chips - 1,)),
        ends_r=dma,
    )
    names = tuple(operands) + tuple(outputs) + tuple(scratch)
    results = pl.pallas_call(
        functools.partial(relay_kernel, names),
        out_shape=[jax.ShapeDtypeStruct(shape, kind) for shape, kind in outputs.values()],
        in_specs=[pl.BlockSpec(memory_space=space(name)) for name in operands],
        out_specs=[
            pl.BlockSpec(memory_space=pl.ANY if name in gathered else pltpu.VMEM)
            for name in outputs
        ],
        scratch_shapes=list(scratch.values()),
        compiler_params=pltpu.CompilerParams(
            collective_id=0, has_side_effects=True, vmem_limit_bytes=60 * 2**20
        ),
        name="relay",
    )(*operands.values())
    return dict(zip(outputs, results))


def weights_kernel(names, *refs):
    r = types.SimpleNamespace(**dict(zip(names, refs)))
    step = pl.program_id(0)
    micro_count, rows, buckets, width = r.activations.shape
    chips, units, head_width = r.ends.shape[0] // 2, r.all_act.shape[-1], r.all_mix.shape[-1]

    @pl.when(step == 0)
    def _():
        sums = r.ends[0]
        for other in range(1, 2 * chips):
            sums = sums + r.ends[other]
        singles = (r.ln1_gain, r.ln1_shift, r.ln2_gain, r.ln2_shift, r.b_out, r.b_proj)
        for place, single in enumerate(singles):
            single[...] = sums[place : place + 1]
        for chip in range(chips):
            both = r.ends[chip] + r.ends[chips + chip]
            r.b_fc[:, chip * units : (chip + 1) * units] = both[6:7, :units]
            here = slice(chip * head_width, (chip + 1) * head_width)
            r.b_qv[0:1, here] = both[7:8, :head_width]
            r.b_qv[1:2, here] = both[7:8, width // 2 : width // 2 + head_width]
        for target, source in ((r.activations, r.acts), (r.in_grads, r.grads)):
            for micro in range(micro_count):
                rows_of = [
                    source[micro * buckets + bucket].astype(F32)[:, None, :]
                    for bucket in range(buckets)
                ]
                target[micro] = jnp.concatenate(rows_of, axis=1).astype(LOW)
        for target in (r.w_qkv, r.w_out, r.w_fc, r.w_proj):
            target[...] = jnp.zeros_like(target)

    def rows_of_sequence(ref):
        return ref[0].reshape(2 * chips * rows, ref.shape[-1])

    nrm, nmlp, ups, brn, act, gpre, mix = (
        rows_of_sequence(ref)
        for ref in (r.all_nrm, r.all_nmlp, r.all_ups, r.all_brn, r.all_act, r.all_gpre, r.all_mix)
    )
    r.w_proj[...] += dot_tn(act, ups)
    r.w_fc[...] += dot_tn(nmlp, gpre)
    r.w_out[...] += dot_tn(mix, brn)
    for which in range(3):
        grad = r.all_dqkv[0, :, which].reshape(2 * chips * rows, head_width)
        r.w_qkv[which] += dot_tn(grad, nrm)


def weights_call(relayed, inputs_shape, head_width, units):
    lines = lax.axis_size("section")
    chips = lax.axis_size("tensor")
    width = inputs_shape[-1]
    half = width // 2
    outputs = dict(
        activations=(inputs_shape, LOW),
        in_grads=(inputs_shape, LOW),
        ln1_gain=((1, width), F32),
        ln1_shift=((1, width), F32),
        w_qkv=((3, head_width, half), F32),
        b_qv=((2, width), F32),
        w_out=((head_width, half), F32),
        b_out=((1, width), F32),
        ln2_gain=((1, width), F32),
        ln2_shift=((1, width), F32),
        w_fc=((half, units), F32),
        b_fc=((1, chips * units), F32),
        w_proj=((units, half), F32),
        b_proj=((1, width), F32),
    )

    def spec(array):
        if len(array.shape) < 5:
            return pl.BlockSpec(array.shape, lambda step: (0,) * len(array.shape))
        return pl.BlockSpec(
            (1,) + array.shape[1:], lambda step: (step,) + (0,) * (len(array.shape) - 1)
        )

    def whole(shape):
        return pl.BlockSpec(shape, lambda step: (0,) * len(shape))

    return pl.pallas_call(
        functools.partial(weights_kernel, tuple(relayed) + tuple(outputs)),
        out_shape=[jax.ShapeDtypeStruct(shape, kind) for shape, kind in outputs.values()],
        grid=(lines,),
        in_specs=[spec(array) for array in relayed.values()],
        out_specs=[whole(shape) for shape, _ in outputs.values()],
        compiler_params=pltpu.CompilerParams(vmem_limit_bytes=60 * 2**20),
        name="weight_gradients",
    )(*relayed.values())


def on_line(
    inputs,
    cotangent,
    lengths,
    chosen,
    ln1_gain,
    ln1_shift,
    w_qkv,
    b_qv,
    w_out,
    b_out,
    ln2_gain,
    ln2_shift,
    w_fc,
    b_fc,
    w_proj,
    b_proj,
):
    head_width, units = w_out.shape[1], w_fc.shape[2]
    singles = dict(
        ln1_gain=ln1_gain,
        ln1_shift=ln1_shift,
        ln2_gain=ln2_gain,
        ln2_shift=ln2_shift,
        b_out=b_out,
        b_proj=b_proj,
        b_fc=b_fc,
        b_qv=b_qv[0],
    )
    weights = dict(
        wq_in=jnp.swapaxes(w_qkv[0], 1, 2).reshape(-1, inputs.shape[-1]),
        wo_in=w_out[0],
        wf_in=w_fc[0],
        wp_in=w_proj[0],
    )
    picks = chosen.reshape((-1,) + chosen.shape[-2:])
    relayed = relay_call(inputs, cotangent, lengths, picks, singles, weights)
    results = list(weights_call(relayed, inputs.shape, head_width, units))
    results[4] = jnp.swapaxes(results[4], 1, 2)
    vectors = (2, 3, 7, 8, 9, 11, 13)
    return tuple(
        result if place in vectors else result[None] for place, result in enumerate(results)
    )


def fits_lines(mesh):
    return mesh.shape["section"] == 4 and mesh.shape["seq"] == 2 and mesh.shape["tensor"] == 4


def solution(mesh):
    placed = (
        P(None, ("seq", "tensor"), None, None),
        P(None, ("seq", "tensor"), None, None),
        P(),
        P("section", None, None, "tensor", "seq", None),
        P("section", None),
        P("section", None),
        P("section", None, None, "tensor"),
        P("section", None, "tensor"),
        P("section", "tensor", None),
        P("section", None),
        P("section", None),
        P("section", None),
        P("section", None, "tensor"),
        P("section", "tensor"),
        P("section", "tensor", None),
        P("section", None),
    )
    return jax.shard_map(
        on_line if fits_lines(mesh) else on_device,
        mesh=mesh,
        in_specs=placed,
        out_specs=(
            P("section", None, ("seq", "tensor"), None, None),
            P("section", None, ("seq", "tensor"), None, None),
            P("section", None),
            P("section", None),
            P("section", None, "seq", "tensor"),
            P("section", None, None),
            P("section", "tensor", "seq"),
            P("section", None),
            P("section", None),
            P("section", None),
            P("section", "seq", "tensor"),
            P("section", None),
            P("section", "tensor", "seq"),
            P("section", None),
        ),
        check_vma=False,
    )
```

```python
import functools
import types

import jax
import jax.numpy as jnp
from jax import lax
from jax.experimental import pallas as pl
from jax.experimental.pallas import tpu as pltpu
from jax.sharding import PartitionSpec as P

HDIM = 64
WIN = 64
QB = 64
KSEL = 64


NORM_EPS = 1e-05
MASKED = -1000000000.0


def from_behind(value, axis, steps):
    count = lax.axis_size(axis)
    first, last = (max(0, -steps), min(count, count - steps))
    return lax.ppermute(value, axis, [(source, source + steps) for source in range(first, last)])


def layer_norm(values, gain, shift):
    average = jnp.mean(values, axis=-1, keepdims=True)
    centred = values - average
    variance = jnp.mean(centred * centred, axis=-1, keepdims=True)
    return centred * lax.rsqrt(variance + NORM_EPS) * gain + shift


def gelu_tanh(values):
    return (
        0.5
        * values
        * (1.0 + jnp.tanh(0.7978845608028654 * (values + 0.044715 * values * values * values)))
    )


def gather_rows(row_block):
    return lax.all_gather(row_block, "tensor", axis=0, tiled=True)


def scatter_product(left_rows, weight, formula):
    return lax.psum_scatter(
        jnp.einsum(formula, left_rows, weight, preferred_element_type=jnp.float32).astype(
            jnp.bfloat16
        ),
        "tensor",
        scatter_dimension=0,
        tiled=True,
    ).astype(jnp.float32)


def near_slabs(full_rows, seq_start, seq_first, length_local):
    buckets = full_rows.shape[1]
    heads_local = full_rows.shape[2] // HDIM
    blocks = length_local // QB
    earlier = lax.dynamic_slice_in_dim(full_rows, jnp.maximum(seq_start - WIN, 0), WIN, 0)
    earlier = jnp.where(seq_first, jnp.zeros_like(earlier), earlier)
    local_part = lax.dynamic_slice_in_dim(full_rows, seq_start, length_local, 0)
    segment = jnp.concatenate([earlier, local_part], 0).reshape(
        length_local + WIN, buckets, heads_local, HDIM
    )
    return jnp.concatenate(
        [
            segment[offset_index * QB : offset_index * QB + length_local].reshape(
                blocks, QB, buckets, heads_local, HDIM
            )
            for offset_index in range(WIN // QB + 1)
        ],
        1,
    )


def far_rows(full_rows, flat_index):
    total_rows, buckets, feature_width = full_rows.shape
    heads_local = feature_width // HDIM
    return jnp.take(full_rows.reshape(total_rows * buckets * heads_local, HDIM), flat_index, axis=0)


def key_geometry(chosen_now, seq_start, blocks):
    buckets, heads_local = (chosen_now.shape[0], chosen_now.shape[1])
    bucket_ids = lax.broadcasted_iota(jnp.int32, chosen_now.shape, 0)
    head_ids = lax.broadcasted_iota(jnp.int32, chosen_now.shape, 1)
    flat_index = (chosen_now * buckets + bucket_ids) * heads_local + head_ids
    block_start = seq_start + QB * lax.broadcasted_iota(jnp.int32, (blocks, 1, 1), 0)
    query_ids = lax.broadcasted_iota(jnp.int32, (1, QB, 1), 1)
    key_ids = lax.broadcasted_iota(jnp.int32, (1, 1, WIN + QB), 2)
    distance = query_ids + WIN - key_ids
    near_ok = (distance >= 0) & (distance < WIN) & (block_start + key_ids - WIN >= 0)
    far_ok = chosen_now + WIN <= block_start.reshape(1, 1, blocks, 1)
    near_mask = jnp.broadcast_to(
        near_ok[:, None, None], (blocks, buckets, heads_local, QB, WIN + QB)
    )
    far_mask = jnp.broadcast_to(
        jnp.transpose(far_ok, (2, 0, 1, 3))[:, :, :, None, :],
        (blocks, buckets, heads_local, QB, KSEL),
    )
    return (flat_index, jnp.concatenate([near_mask, far_mask], -1))


def attention_setup(queries, key_rows, value_rows, chosen_now, seq_start, seq_first):
    length_local, buckets, feature_width = queries.shape
    heads_local = feature_width // HDIM
    blocks = length_local // QB
    query_blocks = queries.reshape(blocks, QB, buckets, heads_local, HDIM)
    flat_index, key_mask = key_geometry(chosen_now, seq_start, blocks)
    near_keys = near_slabs(key_rows, seq_start, seq_first, length_local)
    near_values = near_slabs(value_rows, seq_start, seq_first, length_local)
    far_keys = far_rows(key_rows, flat_index)
    far_values = far_rows(value_rows, flat_index)
    near_scores = jnp.einsum(
        "bqnhe,btnhe->bnhqt", query_blocks, near_keys, preferred_element_type=jnp.float32
    )
    far_scores = jnp.einsum(
        "bqnhe,nhbke->bnhqk", query_blocks, far_keys, preferred_element_type=jnp.float32
    )
    scores = jnp.where(
        key_mask, HDIM ** (-0.5) * jnp.concatenate([near_scores, far_scores], -1), MASKED
    )
    return (query_blocks, near_keys, near_values, far_keys, far_values, flat_index, scores)


def attend(queries, key_rows, value_rows, chosen_now, seq_start, seq_first):
    query_blocks, near_keys, near_values, far_keys, far_values, flat_index, scores = (
        attention_setup(queries, key_rows, value_rows, chosen_now, seq_start, seq_first)
    )
    span = WIN + QB
    row_top = jnp.max(scores, -1, keepdims=True)
    exp_terms = jnp.exp(scores - row_top)
    row_total = jnp.sum(exp_terms, -1, keepdims=True)
    softmax_low = (exp_terms / row_total).astype(jnp.bfloat16)
    near_part = jnp.einsum(
        "bnhqt,btnhe->bqnhe",
        softmax_low[..., :span],
        near_values,
        preferred_element_type=jnp.float32,
    )
    far_part = jnp.einsum(
        "bnhqk,nhbke->bqnhe",
        softmax_low[..., span:],
        far_values,
        preferred_element_type=jnp.float32,
    )
    return ((near_part + far_part).reshape(queries.shape), row_top + jnp.log(row_total))


def spread_back(near_grad, far_grad, flat_index, seq_start, seq_first, total_rows):
    blocks, span, buckets, heads_local, head_size = near_grad.shape
    length_local = blocks * QB
    feature_width = heads_local * head_size
    segment = jnp.zeros((length_local + WIN, buckets, heads_local, head_size), jnp.float32)
    for offset_index in range(WIN // QB + 1):
        piece = near_grad[:, offset_index * QB : (offset_index + 1) * QB].reshape(
            length_local, buckets, heads_local, head_size
        )
        segment = segment.at[offset_index * QB : offset_index * QB + length_local].add(piece)
    full_rows = jnp.zeros((total_rows * buckets * heads_local, head_size), jnp.float32)
    full_rows = full_rows.at[flat_index.reshape(-1)].add(far_grad.reshape(-1, head_size))
    full_rows = full_rows.reshape(total_rows, buckets, feature_width)
    local_part = segment[WIN:].reshape(length_local, buckets, feature_width)
    earlier = jnp.where(seq_first, 0.0, segment[:WIN].reshape(WIN, buckets, feature_width))
    full_rows = lax.dynamic_update_slice_in_dim(
        full_rows,
        lax.dynamic_slice_in_dim(full_rows, seq_start, length_local, 0) + local_part,
        seq_start,
        0,
    )
    earlier_start = jnp.maximum(seq_start - WIN, 0)
    full_rows = lax.dynamic_update_slice_in_dim(
        full_rows,
        lax.dynamic_slice_in_dim(full_rows, earlier_start, WIN, 0) + earlier,
        earlier_start,
        0,
    )
    return full_rows


def attend_back(
    queries, key_rows, value_rows, chosen_now, seq_start, seq_first, log_total, grad_mixed
):
    query_blocks, near_keys, near_values, far_keys, far_values, flat_index, scores = (
        attention_setup(queries, key_rows, value_rows, chosen_now, seq_start, seq_first)
    )
    span = WIN + QB
    score_scale = HDIM ** (-0.5)
    grad_blocks = grad_mixed.reshape(query_blocks.shape)
    weights_full = jnp.exp(scores - log_total)
    softmax_low = weights_full.astype(jnp.bfloat16)
    grad_near_weights = jnp.einsum(
        "bqnhe,btnhe->bnhqt", grad_blocks, near_values, preferred_element_type=jnp.float32
    )
    grad_far_weights = jnp.einsum(
        "bqnhe,nhbke->bnhqk", grad_blocks, far_values, preferred_element_type=jnp.float32
    )
    grad_weights = jnp.concatenate([grad_near_weights, grad_far_weights], -1)
    row_dot = jnp.sum(weights_full * grad_weights, -1, keepdims=True)
    grad_scores = (weights_full * (grad_weights - row_dot)).astype(jnp.bfloat16)
    grad_near, grad_far = (grad_scores[..., :span], grad_scores[..., span:])
    grad_queries = score_scale * (
        jnp.einsum("bnhqt,btnhe->bqnhe", grad_near, near_keys, preferred_element_type=jnp.float32)
        + jnp.einsum("bnhqk,nhbke->bqnhe", grad_far, far_keys, preferred_element_type=jnp.float32)
    )
    near_key_grad = score_scale * jnp.einsum(
        "bnhqt,bqnhe->btnhe", grad_near, query_blocks, preferred_element_type=jnp.float32
    )
    far_key_grad = score_scale * jnp.einsum(
        "bnhqk,bqnhe->nhbke", grad_far, query_blocks, preferred_element_type=jnp.float32
    )
    near_value_grad = jnp.einsum(
        "bnhqt,bqnhe->btnhe",
        softmax_low[..., :span],
        grad_blocks,
        preferred_element_type=jnp.float32,
    )
    far_value_grad = jnp.einsum(
        "bnhqk,bqnhe->nhbke",
        softmax_low[..., span:],
        grad_blocks,
        preferred_element_type=jnp.float32,
    )
    total_rows = key_rows.shape[0]
    key_grad = spread_back(
        near_key_grad, far_key_grad, flat_index, seq_start, seq_first, total_rows
    )
    value_grad = spread_back(
        near_value_grad, far_value_grad, flat_index, seq_start, seq_first, total_rows
    )
    return (grad_queries.reshape(queries.shape), key_grad, value_grad)


def forward_pass(hidden, params, chosen_now, query_mask, seq_start, seq_first, finish):
    (
        ln1_gain,
        ln1_shift,
        w_qkv,
        b_qv,
        w_out,
        b_out,
        ln2_gain,
        ln2_shift,
        w_fc,
        b_fc,
        w_proj,
        b_proj,
    ) = params
    hidden_wide = hidden.astype(jnp.float32)
    normed_all = gather_rows(layer_norm(hidden_wide, ln1_gain, ln1_shift).astype(jnp.bfloat16))
    projected = jnp.einsum("pnd,jdc->jpnc", normed_all, w_qkv, preferred_element_type=jnp.float32)
    queries = (projected[0] + b_qv[0]).astype(jnp.bfloat16)
    key_rows, value_rows = (
        lax.all_gather(projected[1].astype(jnp.bfloat16), "seq", axis=0, tiled=True),
        lax.all_gather((projected[2] + b_qv[1]).astype(jnp.bfloat16), "seq", axis=0, tiled=True),
    )
    attended, log_total = attend(queries, key_rows, value_rows, chosen_now, seq_start, seq_first)
    mixed_rows = (attended * query_mask[:, :, None]).astype(jnp.bfloat16)
    middle = hidden_wide + scatter_product(mixed_rows, w_out, "pnc,cd->pnd") + b_out
    normed_mlp = gather_rows(layer_norm(middle, ln2_gain, ln2_shift).astype(jnp.bfloat16))
    pre_active = (
        jnp.einsum("pnd,df->pnf", normed_mlp, w_fc, preferred_element_type=jnp.float32) + b_fc
    )
    active = gelu_tanh(pre_active).astype(jnp.bfloat16)
    if not finish:
        return (
            normed_all,
            queries,
            key_rows,
            value_rows,
            log_total,
            mixed_rows,
            middle,
            normed_mlp,
            pre_active,
            active,
        )
    output = (middle + scatter_product(active, w_proj, "pnf,fd->pnd") + b_proj).astype(jnp.bfloat16)
    return (output, (key_rows, value_rows))


def backward_pass(hidden, upstream, params, chosen_now, query_mask, seq_start, seq_first):
    (
        ln1_gain,
        ln1_shift,
        w_qkv,
        b_qv,
        w_out,
        b_out,
        ln2_gain,
        ln2_shift,
        w_fc,
        b_fc,
        w_proj,
        b_proj,
    ) = params
    (
        normed_all,
        queries,
        key_rows,
        value_rows,
        log_total,
        mixed_rows,
        middle,
        normed_mlp,
        pre_active,
        active,
    ) = forward_pass(hidden, params, chosen_now, query_mask, seq_start, seq_first, False)
    upstream_all = gather_rows(upstream)
    grad_w_proj = jnp.einsum(
        "pnf,pnd->fd", active, upstream_all, preferred_element_type=jnp.float32
    )
    grad_b_proj = jnp.sum(upstream.astype(jnp.float32), axis=(0, 1))
    grad_active = jnp.einsum(
        "pnd,fd->pnf", upstream_all, w_proj, preferred_element_type=jnp.float32
    )
    unused_value, gelu_pull = jax.vjp(gelu_tanh, pre_active)
    grad_pre = gelu_pull(grad_active)[0].astype(jnp.bfloat16)
    grad_w_fc = jnp.einsum("pnd,pnf->df", normed_mlp, grad_pre, preferred_element_type=jnp.float32)
    grad_b_fc = jnp.sum(grad_pre.astype(jnp.float32), axis=(0, 1))
    grad_normed_mlp = scatter_product(grad_pre, w_fc, "pnf,df->pnd")
    unused_norm, second_pull = jax.vjp(layer_norm, middle, ln2_gain, ln2_shift)
    grad_mid_norm, grad_ln2_gain, grad_ln2_shift = second_pull(grad_normed_mlp)
    grad_middle = upstream.astype(jnp.float32) + grad_mid_norm
    grad_branch = grad_middle.astype(jnp.bfloat16)
    grad_b_out = jnp.sum(grad_branch.astype(jnp.float32), axis=(0, 1))
    branch_all = gather_rows(grad_branch)
    grad_w_out = jnp.einsum(
        "pnc,pnd->cd", mixed_rows, branch_all, preferred_element_type=jnp.float32
    )
    grad_mixed = jnp.einsum(
        "pnd,cd->pnc", branch_all, w_out, preferred_element_type=jnp.float32
    ).astype(jnp.bfloat16) * query_mask[:, :, None].astype(jnp.bfloat16)
    grad_queries, key_grad_all, value_grad_all = attend_back(
        queries, key_rows, value_rows, chosen_now, seq_start, seq_first, log_total, grad_mixed
    )
    key_grad, value_grad = (
        lax.psum_scatter(
            key_grad_all.astype(jnp.bfloat16), "seq", scatter_dimension=0, tiled=True
        ).astype(jnp.float32),
        lax.psum_scatter(
            value_grad_all.astype(jnp.bfloat16), "seq", scatter_dimension=0, tiled=True
        ).astype(jnp.float32),
    )
    grad_project = jnp.stack(
        [
            grad_queries.astype(jnp.bfloat16),
            key_grad.astype(jnp.bfloat16),
            value_grad.astype(jnp.bfloat16),
        ],
        2,
    )
    grad_w_qkv = jnp.einsum(
        "pnd,pnjc->jdc", normed_all, grad_project, preferred_element_type=jnp.float32
    )
    grad_b_qv = jnp.sum(grad_project[:, :, 0::2].astype(jnp.float32), axis=(0, 1))
    grad_normed = scatter_product(grad_project, w_qkv, "pnjc,jdc->pnd")
    unused_first, first_pull = jax.vjp(layer_norm, hidden.astype(jnp.float32), ln1_gain, ln1_shift)
    grad_in_norm, grad_ln1_gain, grad_ln1_shift = first_pull(grad_normed)
    grad_hidden = (grad_middle + grad_in_norm).astype(jnp.bfloat16)
    block_grads = (
        grad_ln1_gain,
        grad_ln1_shift,
        grad_w_qkv,
        grad_b_qv,
        grad_w_out,
        grad_b_out,
        grad_ln2_gain,
        grad_ln2_shift,
        grad_w_fc,
        grad_b_fc,
        grad_w_proj,
        grad_b_proj,
    )
    return (grad_hidden, block_grads)


def on_device(
    inputs,
    cotangent,
    lengths,
    chosen,
    ln1_gain,
    ln1_shift,
    w_qkv,
    b_qv,
    w_out,
    b_out,
    ln2_gain,
    ln2_shift,
    w_fc,
    b_fc,
    w_proj,
    b_proj,
):
    params = tuple(
        (
            weight_array[0]
            for weight_array in (
                ln1_gain,
                ln1_shift,
                w_qkv,
                b_qv,
                w_out,
                b_out,
                ln2_gain,
                ln2_shift,
                w_fc,
                b_fc,
                w_proj,
                b_proj,
            )
        )
    )
    section_index = lax.axis_index("section")
    section_count = lax.axis_size("section")
    seq_index = lax.axis_index("seq")
    tensor_index = lax.axis_index("tensor")
    tensor_count = lax.axis_size("tensor")
    micro_count, rows_local, buckets, feature_width = inputs.shape
    length_local = rows_local * tensor_count
    heads_width = w_qkv.shape[-1]
    seq_start = seq_index * length_local
    seq_first = seq_index == 0
    positions = seq_start + lax.broadcasted_iota(jnp.int32, (micro_count, length_local, buckets), 1)
    mask_all = (positions < lengths[:, None, :]).astype(jnp.float32)
    mask_rows = lax.dynamic_slice_in_dim(mask_all, tensor_index * rows_local, rows_local, 1)
    step_count = micro_count + section_count - 1
    chosen_section = chosen[0]
    received = jnp.zeros((rows_local, buckets, feature_width), jnp.bfloat16)
    stored = jnp.zeros((micro_count, rows_local, buckets, feature_width), jnp.bfloat16)
    outputs = jnp.zeros_like(stored)
    for step_index in range(step_count):
        micro_index = step_index - section_index
        running = (micro_index >= 0) & (micro_index < micro_count)
        slot_index = jnp.clip(micro_index, 0, micro_count - 1)
        block_in = jnp.where(
            section_index == 0, lax.dynamic_index_in_dim(inputs, slot_index, 0, False), received
        )
        chosen_now = lax.dynamic_index_in_dim(chosen_section, slot_index, 0, False)
        query_mask = lax.dynamic_index_in_dim(mask_all, slot_index, 0, False)
        result, key_pair = forward_pass(
            block_in, params, chosen_now, query_mask, seq_start, seq_first, True
        )
        stored = jnp.where(
            running, lax.dynamic_update_index_in_dim(stored, block_in, slot_index, 0), stored
        )
        outputs = jnp.where(
            running, lax.dynamic_update_index_in_dim(outputs, result, slot_index, 0), outputs
        )
        received = from_behind(result, "section", 1)
    back_received = jnp.zeros((rows_local, buckets, feature_width), jnp.bfloat16)
    in_grads = jnp.zeros_like(stored)
    totals = None
    for step_index in range(step_count):
        micro_index = step_index - (section_count - 1 - section_index)
        running = (micro_index >= 0) & (micro_index < micro_count)
        slot_index = jnp.clip(micro_index, 0, micro_count - 1)
        chosen_now = lax.dynamic_index_in_dim(chosen_section, slot_index, 0, False)
        query_mask = lax.dynamic_index_in_dim(mask_all, slot_index, 0, False)
        local_mask = lax.dynamic_index_in_dim(mask_rows, slot_index, 0, False)
        top_grad = (
            lax.dynamic_index_in_dim(cotangent, slot_index, 0, False).astype(jnp.float32)
            * local_mask[:, :, None]
        ).astype(jnp.bfloat16)
        upstream = jnp.where(section_index == section_count - 1, top_grad, back_received)
        hidden = lax.dynamic_index_in_dim(stored, slot_index, 0, False)
        grad_hidden, block_grads = backward_pass(
            hidden, upstream, params, chosen_now, query_mask, seq_start, seq_first
        )
        block_grads = tuple(
            (jnp.where(running, grad_part, jnp.zeros_like(grad_part)) for grad_part in block_grads)
        )
        totals = (
            block_grads
            if step_index == 0
            else tuple(
                (total_part + grad_part for total_part, grad_part in zip(totals, block_grads))
            )
        )
        in_grads = jnp.where(
            running, lax.dynamic_update_index_in_dim(in_grads, grad_hidden, slot_index, 0), in_grads
        )
        back_received = from_behind(grad_hidden, "section", -1)
    (
        sum_ln1_gain,
        sum_ln1_shift,
        sum_w_qkv,
        sum_b_qv,
        sum_w_out,
        sum_b_out,
        sum_ln2_gain,
        sum_ln2_shift,
        sum_w_fc,
        sum_b_fc,
        sum_w_proj,
        sum_b_proj,
    ) = totals
    part_qkv, part_out, part_fc, part_proj = (
        lax.psum_scatter(
            sum_w_qkv.astype(jnp.bfloat16), "seq", scatter_dimension=1, tiled=True
        ).astype(jnp.float32),
        lax.psum_scatter(
            sum_w_out.astype(jnp.bfloat16), "seq", scatter_dimension=1, tiled=True
        ).astype(jnp.float32),
        lax.psum_scatter(
            sum_w_fc.astype(jnp.bfloat16), "seq", scatter_dimension=0, tiled=True
        ).astype(jnp.float32),
        lax.psum_scatter(
            sum_w_proj.astype(jnp.bfloat16), "seq", scatter_dimension=1, tiled=True
        ).astype(jnp.float32),
    )
    bias_qv = lax.dynamic_update_slice_in_dim(
        jnp.zeros((2, feature_width), jnp.float32), sum_b_qv, tensor_index * heads_width, 1
    )
    units_local = sum_b_fc.shape[0]
    bias_fc = lax.dynamic_update_slice_in_dim(
        jnp.zeros((units_local * tensor_count,), jnp.float32),
        sum_b_fc,
        tensor_index * units_local,
        0,
    )
    small_sums = lax.psum(
        (
            sum_ln1_gain,
            sum_ln1_shift,
            bias_qv,
            sum_b_out,
            sum_ln2_gain,
            sum_ln2_shift,
            bias_fc,
            sum_b_proj,
        ),
        ("seq", "tensor"),
    )
    return (
        outputs[None],
        in_grads[None],
        small_sums[0][None],
        small_sums[1][None],
        part_qkv[None],
        small_sums[2][None],
        part_out[None],
        small_sums[3][None],
        small_sums[4][None],
        small_sums[5][None],
        part_fc[None],
        small_sums[6][None],
        part_proj[None],
        small_sums[7][None],
    )


STREAMS = 2
NRM, NMLP, UPS, BRN, ACT, GPRE, MIX, DQKV = range(8)
F32 = jnp.float32
LOW = jnp.bfloat16
MESH_ID = pl.DeviceIdType.MESH


def dot_nn(left, right):
    return lax.dot_general(left, right, (((1,), (0,)), ((), ())), preferred_element_type=F32)


def dot_nt(left, right):
    return lax.dot_general(left, right, (((1,), (1,)), ((), ())), preferred_element_type=F32)


def dot_tn(left, right):
    return lax.dot_general(left, right, (((0,), (0,)), ((), ())), preferred_element_type=F32)


def standard(rows):
    centred = rows - jnp.mean(rows, axis=-1, keepdims=True)
    scale = lax.rsqrt(jnp.mean(centred * centred, axis=-1, keepdims=True) + NORM_EPS)
    return centred * scale, scale


def standard_back(grad, xhat, scale):
    inner = jnp.mean(grad * xhat, axis=-1, keepdims=True)
    return scale * (grad - jnp.mean(grad, axis=-1, keepdims=True) - xhat * inner)


def column_sum(rows):
    return jnp.sum(rows.astype(F32), axis=0, keepdims=True)


def relay_kernel(names, *refs):
    r = types.SimpleNamespace(**dict(zip(names, refs)))
    a, c, t = (lax.axis_index(name) for name in ("section", "seq", "tensor"))
    lines = lax.axis_size("section")
    chips = lax.axis_size("tensor")
    rows, buckets, width = r.inputs.shape[1:]
    half_width = width // 2
    local = rows * chips
    total = 2 * local
    stream_rows = local // STREAMS
    head_width = r.wo_in.shape[0]
    heads = head_width // HDIM
    blocks = local // QB
    units = r.wp_in.shape[0]
    scale = HDIM ** (-0.5)
    streams = range(STREAMS)

    def remote(src, dst, send, recv, **target):
        return pltpu.make_async_remote_copy(
            src_ref=src,
            dst_ref=dst,
            send_sem=send,
            recv_sem=recv,
            device_id=target,
            device_id_type=MESH_ID,
        )

    def drain(ref, sem):
        pltpu.make_async_copy(ref, ref, sem).wait()

    def row_block(index, size):
        return pl.ds(pl.multiple_of(index * size, size), size)

    near_chip = t + 1 - 2 * (t % 2)
    over_chip = (t + 2) % 4
    across_chip = 3 - t
    middle_chip = (t == 1) | (t == 2)
    end_chip = (t == 0) | (t == 3)
    owned = stream_rows // 2
    mine = row_block(t - 1, owned)
    my_half = row_block(c, local)

    r.kv[...] = jnp.zeros(r.kv.shape, LOW)

    barrier = pltpu.get_barrier_semaphore()
    greeted = 0
    for line in range(lines):
        for chip in range(chips):
            for core in range(2):
                if (line, chip, core) != (0, 0, 0) and (core == 0 or line * chip == 0):
                    there = {
                        "section": (a + line) % lines,
                        "seq": (c + core) % 2,
                        "tensor": (t + chip) % chips,
                    }
                    pl.semaphore_signal(barrier, inc=1, device_id=there, device_id_type=MESH_ID)
                    greeted += 1
    pl.semaphore_wait(barrier, greeted)

    def beside(s):
        return s + 1 - 2 * (s % 2)

    def above(s):
        return (s + 2) % 4

    def store(p):
        return (r.wq, r.wo, r.wf, r.wp)[p]

    def source(p):
        return (r.wq_in, r.wo_in, r.wf_in, r.wp_in)[p]

    def height(p):
        return source(p).shape[0]

    def core_half(p, s, core):
        return store(p).at[s, row_block(core, height(p) // 2)]

    def first_hop(p, s, neighbour, which):
        return remote(
            source(p).at[row_block(c, height(p) // 2)],
            core_half(p, s, c),
            r.w_first_s.at[p, which],
            r.w_first_r.at[s, p],
            section=neighbour,
        )

    def second_hop(p, s, which):
        view = store(p).at[s, row_block(2 * c + which, height(p) // 4)]
        return remote(
            view, view, r.w_second_s.at[s, p], r.w_second_r.at[s, p, which], section=3 - s
        )

    def core_hop(p, s, core):
        view = core_half(p, s, core)
        return remote(view, view, r.w_core_s.at[s, p], r.w_core_r.at[s, p], seq=1 - c)

    def own_copy(p):
        return pltpu.make_async_copy(source(p), store(p).at[a], r.w_own.at[p])

    def pass_on(s, p, which):
        line = (beside(s), above(s))[which]

        @pl.when(a == line)
        def _():
            first_hop(p, s, line, which).wait_recv()
            second_hop(p, s, which).start()
            core_hop(p, s, c).start()

    def pass_all(s, pieces):
        for p in pieces:
            for which in range(2):
                pass_on(s, p, which)

    def pass_far(s, p):
        @pl.when(a == 3 - s)
        def _():
            second_hop(p, s, 0).wait_recv()
            second_hop(p, s, 1).wait_recv()
            core_hop(p, s, c).start()

    def need(s, p):
        @pl.when(s == 0)
        def _():
            if p < 2:
                pass_all(0, (p,))
            pass_far(0, p)

        @pl.when(a == s)
        def _():
            own_copy(p).wait()

        @pl.when(a != s)
        def _():
            core_hop(p, s, 1 - c).wait_recv()

    def small_copy(step, line, slot):
        return remote(
            r.small_own, r.small.at[slot], r.small_s.at[step], r.small_r.at[slot], section=line
        )

    def count_copy(step, line, slot):
        return remote(
            r.count_own.at[line],
            r.count.at[slot],
            r.count_s.at[step],
            r.count_r.at[slot],
            section=line,
        )

    singles = (r.ln1_gain, r.ln1_shift, r.ln2_gain, r.ln2_shift, r.b_out, r.b_proj)
    for place, single in enumerate(singles):
        r.small_own[place : place + 1] = single[...]
    r.small_own[6:7, :units] = r.b_fc[...]
    r.small_own[7:8, :head_width] = r.b_qv[0:1]
    r.small_own[7:8, half_width : half_width + head_width] = r.b_qv[1:2]
    for step in range(1, lines):
        small_copy(step - 1, (a + step) % lines, a).start()
    for p in range(4):
        for which, line in enumerate((beside(a), above(a))):
            first_hop(p, a, line, which).start()
    for p in range(4):
        own_copy(p).start()
    r.small[a] = r.small_own[...]

    def iota(shape, dimension):
        return lax.broadcasted_iota(jnp.int32, shape, dimension)

    square = jnp.where(iota((KSEL, KSEL), 0) == iota((KSEL, KSEL), 1), 1.0, 0.0).astype(LOW)
    position = iota((KSEL, total), 1).astype(F32)
    for pair in range(lines * heads):
        line, head = pair // heads, pair % heads
        columns = dot_nt(square, r.chosen[pair].astype(F32).astype(LOW))
        for block in range(blocks):
            pick = head * blocks + block
            r.count_own[line, pick : pick + 1, :] = jnp.sum(
                jnp.where(columns[:, block : block + 1] == position, 1.0, 0.0),
                axis=0,
                keepdims=True,
            )
    for step in range(1, lines):
        count_copy(step - 1, (a + step) % lines, a).start()
    r.count[a] = r.count_own[a]

    NEAR, OVER, ACROSS = range(3)

    def gather(buffer, s, kind, j, owner, target, slot):
        view = buffer.at[s, j, row_block(owner - 1, owned)]
        return remote(
            view, view, r.ag_s.at[kind, j, slot], r.ag_r.at[kind, j, slot], tensor=target
        )

    def used_before(s, kind):
        return s > 0 if kind < 2 else s < lines - 1

    def gather_start(buffer, s, kind, j):
        @pl.when(used_before(s, kind))
        def _():
            gather_sent(buffer, s, kind, j)

        gather(buffer, s, kind, j, t, over_chip, OVER).start()
        gather(buffer, s, kind, j, t, across_chip, ACROSS).start()
        gather(buffer, s, kind, j, t, near_chip, NEAR).start()

    def gather_wait(buffer, s, kind, j):
        @pl.when(middle_chip)
        def _():
            gather(buffer, s, kind, j, across_chip, across_chip, ACROSS).wait_recv()

        @pl.when(end_chip)
        def _():
            gather(buffer, s, kind, j, near_chip, near_chip, NEAR).wait_recv()
            gather(buffer, s, kind, j, over_chip, over_chip, OVER).wait_recv()

    def gather_sent(buffer, s, kind, j):
        gather(buffer, s, kind, j, t, over_chip, OVER).wait_send()
        gather(buffer, s, kind, j, t, across_chip, ACROSS).wait_send()
        gather(buffer, s, kind, j, t, near_chip, NEAR).wait_send()

    def scatter(s, kind, j, owner, slot):
        return remote(
            r.part.at[kind, j, row_block(owner - 1, owned)],
            r.arrived.at[s, kind, j, slot],
            r.rs_s.at[kind, j, slot],
            r.rs_r.at[kind, j, slot],
            tensor=owner,
        )

    def scatter_start(s, kind, j, product):
        @pl.when(used_before(s, kind))
        def _():
            scatter_sent(s, kind, j)

        r.part[kind, j] = product.astype(LOW)

        @pl.when(end_chip)
        def _():
            scatter(s, kind, j, over_chip, OVER).start()
            scatter(s, kind, j, near_chip, NEAR).start()

        @pl.when(middle_chip)
        def _():
            scatter(s, kind, j, across_chip, ACROSS).start()

    def scatter_sum(s, kind, j):
        result = r.part[kind, j, mine].astype(F32)
        for slot in (NEAR, ACROSS, OVER):
            scatter(s, kind, j, t, slot).wait_recv()
            result = result + r.arrived[s, kind, j, slot].astype(F32)
        return result

    def scatter_sent(s, kind, j):
        @pl.when(end_chip)
        def _():
            scatter(s, kind, j, over_chip, OVER).wait_send()
            scatter(s, kind, j, near_chip, NEAR).wait_send()

        @pl.when(middle_chip)
        def _():
            scatter(s, kind, j, across_chip, ACROSS).wait_send()

    own_rows = (r.nrm, r.nmlp, r.ups, r.brn, r.act, r.gpre, r.mix, r.dqkv)
    all_rows = (
        r.all_nrm,
        r.all_nmlp,
        r.all_ups,
        r.all_brn,
        r.all_act,
        r.all_gpre,
        r.all_mix,
        r.all_dqkv,
    )

    def rows_copy(index, s, same, stays=False):
        core = c if same else 1 - c
        src = own_rows[index].at[s]
        dst = all_rows[index].at[a, c]
        if index <= BRN:
            src = src.at[:, :, row_block(core, half_width)]
        recv = r.heads_r.at[a] if index == DQKV else r.rows_r.at[index]
        if stays:
            return pltpu.make_async_copy(src, dst, recv)
        if same:
            return remote(src, dst, r.rows_s.at[index, s, 0], recv, section=s)
        return remote(src, dst, r.rows_s.at[index, s, 1], recv, section=s, seq=1 - c)

    passed_rows = {UPS: r.pass_ups, GPRE: r.pass_gpre}
    places = {UPS: 0, GPRE: 1}

    def detour_copy(index):
        return remote(
            own_rows[index].at[0],
            passed_rows[index],
            r.pass_s.at[places[index]],
            r.pass_r.at[places[index]],
            section=1,
        )

    def passed_copies(index):
        copies = []
        for step in range(2 if index <= BRN else 1):
            core = (c + step) % 2
            src = passed_rows[index]
            if index <= BRN:
                src = src.at[:, :, row_block(core, half_width)]
            send = r.pass_on_s.at[places[index], step]
            dst = all_rows[index].at[3, c]
            copies.append(remote(src, dst, send, r.rows_r.at[index], section=0, seq=core))
        return copies

    def pass_rows(index):
        @pl.when(a == 1)
        def _():
            detour_copy(index).wait_recv()
            for copy in passed_copies(index):
                copy.start()

    def goes_direct(index, s):
        return jnp.logical_not((a == 3) & (s == 0)) if index in passed_rows else a >= 0

    def rows_start(index, s):
        if index in passed_rows:

            @pl.when((a == 3) & (s == 0))
            def _():
                detour_copy(index).start()

        @pl.when(a == s)
        def _():
            rows_copy(index, s, True, True).start()

        @pl.when((a != s) & goes_direct(index, s))
        def _():
            rows_copy(index, s, True).start()

        if index <= BRN:

            @pl.when(goes_direct(index, s))
            def _():
                rows_copy(index, s, False).start()

    def forward_rows(s):
        for index in (NRM, MIX, NMLP, ACT):
            rows_start(index, s)

    def rows_sent(index, s):
        @pl.when((a != s) & goes_direct(index, s))
        def _():
            rows_copy(index, s, True).wait_send()

        if index <= BRN:

            @pl.when(goes_direct(index, s))
            def _():
                rows_copy(index, s, False).wait_send()

    def share_copy(index, core):
        view = all_rows[index].at[:, core]
        return remote(view, view, r.share_s.at[index - ACT], r.share_r.at[index - ACT], seq=1 - c)

    def share_heads(line, core):
        view = r.all_dqkv.at[line, core]
        return remote(view, view, r.heads_s.at[line], r.heads_sr.at[line], seq=1 - c)

    def share(index):
        drain(all_rows[index].at[:, c], r.rows_r.at[index])
        share_copy(index, c).start()

    def norm_copy(s):
        return remote(
            r.norm_part.at[s], r.norm_all.at[a], r.norm_s.at[s], r.norm_r, section=s
        )

    def norm_start(s):
        @pl.when(a == s)
        def _():
            pltpu.make_async_copy(r.norm_part.at[s], r.norm_all.at[a], r.norm_r).start()

        @pl.when(a != s)
        def _():
            norm_copy(s).start()

    def home_copy(what, s, j):
        src, dst, send, recv = what
        chip = 2 * j + t - 1
        return remote(src.at[s, j], dst.at[a], send.at[s, j], recv, section=s, tensor=chip)

    def home_start(what, s):
        @pl.when(middle_chip)
        def _():
            for j in streams:
                home_copy(what, s, j).start()

    def home_sent(what, s):
        @pl.when(middle_chip)
        def _():
            for j in streams:
                home_copy(what, s, j).wait_send()

    out_home = (r.out_low, r.acts, r.out_s, r.out_r)
    grad_home = (r.grad_low, r.grads, r.grad_s, r.grad_r)

    length = r.lengths[a // buckets, a % buckets]
    key = iota((stream_rows, total), 1)
    for j in streams:
        query = c * local + j * stream_rows + iota((stream_rows, total), 0)
        r.near[j] = jnp.where((query >= key) & (query - key < WIN), 1.0, 0.0)
    key_row = iota((1, total), 1)

    def row_mask(place):
        return jnp.where(place < length, 1.0, 0.0)

    def stream_mask(j):
        return row_mask(c * local + j * stream_rows + iota((stream_rows, 1), 0))

    def multiplicity(s, j, head):
        block = j * stream_rows // QB
        pick = head * blocks + block
        limit = (c * blocks + block) * QB - WIN
        return r.near[j] + jnp.where(key_row <= limit, r.count[s, pick : pick + 1, :], 0.0)

    def head_cols(head):
        return slice(head * HDIM, (head + 1) * HDIM)

    def kv_copy(s, j):
        view = r.kv.at[s, :, j * stream_rows : (j + 1) * stream_rows]
        return remote(view, view, r.kv_s.at[s, j], r.kv_r.at[s, j], seq=1 - c)

    def dkv_copy(s):
        return remote(r.dkv_out.at[s], r.dkv_in.at[s], r.dkv_s.at[s], r.dkv_r.at[s], seq=1 - c)

    def own_sequence(ref):
        both = ref[a // buckets].astype(F32)
        picked = both[:, 0, :]
        for bucket in range(1, buckets):
            picked = jnp.where(a % buckets == bucket, both[:, bucket, :], picked)
        return picked

    def first_copy(stream):
        return remote(
            r.first_out, r.first_in.at[stream], r.first_s, r.first_r.at[stream], tensor=1 + t % 2
        )

    own_place = c * local + t * rows + iota((rows, 1), 0)
    r.first_out[0] = own_sequence(r.inputs).astype(LOW)
    r.first_out[1] = (own_sequence(r.cotangent) * row_mask(own_place)).astype(LOW)
    first_copy(t // 2).start()
    r.norm_part[...] = jnp.zeros_like(r.norm_part)

    def first_rows(j):
        @pl.when(middle_chip)
        def _():
            first_copy(j).wait_recv()
            r.hidden[j] = r.first_in[j, 0].astype(F32)
            r.upstream[j] = r.first_in[j, 1]

    def on_owner(stage):
        def run(s, j):
            @pl.when(middle_chip)
            def _():
                stage(s, j)

        return run

    @on_owner
    def enter(s, j):
        xhat, inverse = standard(r.hidden[j])
        r.xhat1[s, j] = xhat
        r.inv1[s, j] = jnp.broadcast_to(inverse, (owned, 128))
        r.nrm[s, j, mine] = (xhat * r.small[s, 0:1] + r.small[s, 1:2]).astype(LOW)
        gather_start(r.nrm, s, 0, j)

    def project(s, j):
        gather_wait(r.nrm, s, 0, j)
        normed = r.nrm[s, j]
        place = row_block(c * STREAMS + j, stream_rows)
        bias_v = r.small[s, 7:8, half_width : half_width + head_width]
        key_rows = dot_nt(normed, r.wq[s, head_width : 2 * head_width])
        value_rows = dot_nt(normed, r.wq[s, 2 * head_width : 3 * head_width]) + bias_v
        r.kv[s, 0, place] = key_rows.astype(LOW)
        r.kv[s, 1, place] = value_rows.astype(LOW)

    def ask(s, j):
        queries = dot_nt(r.nrm[s, j], r.wq[s, 0:head_width]) + r.small[s, 7:8, :head_width]
        r.qry[s, j] = queries.astype(LOW)

    def attend_line(s, j):
        mixed = []
        for head in range(heads):
            cols = head_cols(head)
            times = multiplicity(s, j, head)
            scores = scale * dot_nt(r.qry[s, j, :, cols], r.kv[s, 0, :, cols])
            scores = jnp.where(times > 0.0, scores, MASKED)
            top = jnp.max(scores, axis=-1, keepdims=True)
            terms = times * jnp.exp(scores - top)
            weights = terms / jnp.sum(terms, axis=-1, keepdims=True)
            r.soft[s, j, head] = weights
            mixed.append(dot_nn(weights.astype(LOW), r.kv[s, 1, :, cols]))
        r.mix[s, j] = (jnp.concatenate(mixed, axis=-1) * stream_mask(j)).astype(LOW)

    def leave_attention(s, j):
        scatter_start(s, 0, j, dot_nn(r.mix[s, j], r.wo[s]))

    @on_owner
    def between(s, j):
        middle = r.hidden[j] + scatter_sum(s, 0, j) + r.small[s, 4:5]
        r.middle[j] = middle
        xhat, inverse = standard(middle)
        r.xhat2[s, j] = xhat
        r.inv2[s, j] = jnp.broadcast_to(inverse, (owned, 128))
        r.nmlp[s, j, mine] = (xhat * r.small[s, 2:3] + r.small[s, 3:4]).astype(LOW)
        gather_start(r.nmlp, s, 1, j)

    def feed(s, j):
        gather_wait(r.nmlp, s, 1, j)
        before = dot_nn(r.nmlp[s, j], r.wf[s]) + r.small[s, 6:7, :units]
        bend = jnp.tanh(0.7978845608028654 * (before + 0.044715 * before * before * before))
        r.act[s, j] = (0.5 * before * (1.0 + bend)).astype(LOW)
        r.slope[s, j] = 0.5 * (1.0 + bend) + 0.5 * before * (1.0 - bend * bend) * (
            0.7978845608028654 * (1.0 + 3 * 0.044715 * before * before)
        )


    def leave_feed(s, j):
        scatter_start(s, 1, j, dot_nn(r.act[s, j], r.wp[s]))

    @on_owner
    def finish(s, j):
        result = r.middle[j] + scatter_sum(s, 1, j) + r.small[s, 5:6]
        r.out_low[s, j] = result.astype(LOW)
        r.hidden[j] = result.astype(LOW).astype(F32)

    def small_ready(s):
        @pl.when(a != s)
        def _():
            small_copy(0, a, s).wait_recv()

    small_ready(0)
    for j in streams:
        first_rows(j)
        enter(0, j)

    def forward(s, _):
        need(s, 0)
        need(s, 1)

        @pl.when(a != s)
        def _():
            count_copy(0, a, s).wait_recv()

        for j in streams:
            project(s, j)

            @pl.when(c == 0)
            def _():
                kv_copy(s, j).start()

            ask(s, j)
            if j == 0:

                @pl.when(c == 1)
                def _():
                    for other in streams:
                        kv_copy(s, other).wait_recv()

            attend_line(s, j)
            leave_attention(s, j)

        @pl.when(s == 0)
        def _():
            pass_all(0, (2,))
            for later in range(1, lines):
                pass_all(later, (0, 1, 2))

        @pl.when(s == 1)
        def _():
            pass_far(1, 2)
            pass_far(1, 3)
            for later in range(2, lines):
                for p in range(4):
                    pass_far(later, p)

        for j in streams:
            between(s, j)
        @pl.when(s == 0)
        def _():
            for later in range(lines):
                pass_all(later, (3,))

        need(s, 2)
        for j in streams:
            feed(s, j)
            if j == 0:
                need(s, 3)
            leave_feed(s, j)


        @pl.when(s >= 2)
        def _():
            forward_rows(s - 2)


        @pl.when(s + 1 < lines)
        def _():
            small_ready(s + 1)

        for j in streams:
            finish(s, j)

            @pl.when(s + 1 < lines)
            def _():
                enter(s + 1, j)

        home_start(out_home, s)

        @pl.when(s == 0)
        def _():
            pass_far(1, 0)
            pass_far(1, 1)

        return 0

    lax.fori_loop(0, lines, forward, 0)

    @on_owner
    def turn(s, j):
        upstream = r.upstream[j]
        r.ups[s, j, mine] = upstream
        gather_start(r.ups, s, 2, j)
        r.norm_part[s, 5:6] += column_sum(upstream)

    def feed_back(s, j):
        gather_wait(r.ups, s, 2, j)
        grad_pre = (dot_nt(r.ups[s, j], r.wp[s]) * r.slope[s, j]).astype(LOW)
        r.gpre[s, j] = grad_pre
        scatter_start(s, 2, j, dot_nt(grad_pre, r.wf[s]))
        r.norm_part[s, 6:7, :units] += column_sum(grad_pre)

    @on_owner
    def between_back(s, j):
        grad = scatter_sum(s, 2, j)
        xhat = r.xhat2[s, j]
        upstream = r.upstream[j].astype(F32)
        grad_middle = upstream + standard_back(
            grad * r.small[s, 2:3], xhat, r.inv2[s, j, :, 0:1]
        )
        r.middle[j] = grad_middle
        branch = grad_middle.astype(LOW)
        r.brn[s, j, mine] = branch
        gather_start(r.brn, s, 3, j)
        r.norm_part[s, 2:3] += column_sum(grad * xhat)
        r.norm_part[s, 3:4] += column_sum(grad)
        r.norm_part[s, 4:5] += column_sum(branch)

    def mixed_back(s, j):
        gather_wait(r.brn, s, 3, j)
        r.gmix[j] = (dot_nt(r.brn[s, j], r.wo[s]) * stream_mask(j)).astype(LOW)

    def attend_line_back(s, j):
        grad_q, grad_k, grad_v = [], [], []
        for head in range(heads):
            cols = head_cols(head)
            weights = r.soft[s, j, head]
            grad_head = r.gmix[j, :, cols]
            grad_weights = dot_nt(grad_head, r.kv[s, 1, :, cols])
            inner = jnp.sum(weights * grad_weights, axis=-1, keepdims=True)
            grad_scores = (weights * (grad_weights - inner)).astype(LOW)
            grad_k.append(scale * dot_tn(grad_scores, r.qry[s, j, :, cols]))
            grad_v.append(dot_tn(weights.astype(LOW), grad_head))
            grad_q.append(scale * dot_nn(grad_scores, r.kv[s, 0, :, cols]))
        for which, grad in enumerate((grad_k, grad_v)):
            grad = jnp.concatenate(grad, axis=-1)
            r.dkv_all[which] = grad if j == STREAMS - 1 else r.dkv_all[which] + grad
        grad_q = jnp.concatenate(grad_q, axis=-1).astype(LOW)
        r.dqkv[s, 0, j] = grad_q
        r.norm_part[s, 7:8, :head_width] += column_sum(grad_q)

    def join_keys(s, j):
        for which in range(2):
            joined = r.dkv_all[which, row_block(c * STREAMS + j, stream_rows)].astype(LOW)
            r.dqkv[s, 1 + which, j] = joined
            if which == 1:
                lanes = slice(half_width, half_width + head_width)
                r.norm_part[s, 7:8, lanes] += column_sum(joined)

    def leave_back(s, j):
        product = dot_nn(r.dqkv[s, 0, j], r.wq[s, 0:head_width])
        for which in range(1, 3):
            weight = r.wq[s, which * head_width : (which + 1) * head_width]
            product = product + dot_nn(r.dqkv[s, which, j], weight)
        scatter_start(s, 3, j, product)

    @on_owner
    def finish_back(s, j):
        grad = scatter_sum(s, 3, j)
        xhat = r.xhat1[s, j]
        result = r.middle[j] + standard_back(
            grad * r.small[s, 0:1], xhat, r.inv1[s, j, :, 0:1]
        )
        r.upstream[j] = result.astype(LOW)
        r.grad_low[s, j] = result.astype(LOW)
        r.norm_part[s, 0:1] += column_sum(grad * xhat)
        r.norm_part[s, 1:2] += column_sum(grad)

    last_first = tuple(reversed(streams))
    for j in last_first:
        turn(lines - 1, j)

    def backward(index, _):
        s = lines - 1 - index
        for j in last_first:
            feed_back(s, j)
        rows_start(UPS, s)
        rows_start(GPRE, s)

        @pl.when(index < 2)
        def _():
            forward_rows(lines - 2 + index)

        @pl.when(index == lines - 1)
        def _():
            share(ACT)
            share(MIX)

        for j in last_first:
            between_back(s, j)
        for j in last_first:
            mixed_back(s, j)
            if j == 0:
                rows_start(BRN, s)
            attend_line_back(s, j)

            @pl.when(c == 1)
            def _():
                join_keys(s, j)
                leave_back(s, j)

        @pl.when(c == 1)
        def _():
            r.dkv_out[s] = r.dkv_all[:, 0:local].astype(LOW)
            dkv_copy(s).start()

        @pl.when(c == 0)
        def _():
            dkv_copy(s).wait_recv()
            r.dkv_all[:, 0:local] += r.dkv_in[s].astype(F32)
            for j in last_first:
                join_keys(s, j)
                leave_back(s, j)

        rows_start(DQKV, s)

        @pl.when(s == 0)
        def _():
            pass_rows(UPS)
            pass_rows(GPRE)

        for j in last_first:
            finish_back(s, j)

            @pl.when(s > 0)
            def _():
                turn(s - 1, j)

        norm_start(s)
        home_start(grad_home, s)
        return 0

    lax.fori_loop(0, lines, backward, 0)

    share(GPRE)
    for line in range(lines):
        drain(r.all_dqkv.at[line, c], r.heads_r.at[line])
        share_heads(line, c).start()

    drain(r.norm_all, r.norm_r)
    slot = c * chips + t
    norm_sum = r.norm_all[0]
    for line in range(1, lines):
        norm_sum = norm_sum + r.norm_all[line]
    r.ends[slot] = norm_sum

    def ends_copy(step):
        core, chip = step // chips, step % chips
        view = r.ends.at[slot]
        return remote(
            view,
            view,
            r.ends_s.at[step - 1],
            r.ends_r,
            seq=(c + core) % 2,
            tensor=(t + chip) % chips,
        )

    for step in range(1, 2 * chips):
        ends_copy(step).start()

    for index in (UPS, GPRE):

        @pl.when(a == 3)
        def _():
            detour_copy(index).wait_send()

        @pl.when(a == 1)
        def _():
            for copy in passed_copies(index):
                copy.wait_send()

    for kind, buffer in enumerate((r.nrm, r.nmlp, r.ups, r.brn)):
        for j in streams:
            scatter_sent(0, kind, j)

            @pl.when(middle_chip)
            def _():
                gather_sent(buffer, 0, kind, j)

    for index in range(ACT):
        drain(all_rows[index], r.rows_r.at[index])
    for index in range(ACT, DQKV):
        share_copy(index, 1 - c).wait_recv()
        share_copy(index, c).wait_send()
    for line in range(lines):
        share_heads(line, 1 - c).wait_recv()
        share_heads(line, c).wait_send()
    drain(r.acts, r.out_r)
    drain(r.grads, r.grad_r)
    drain(r.ends.at[0 : 2 * chips - 1], r.ends_r)
    for step in range(1, 2 * chips):
        ends_copy(step).wait_send()
    for step in range(1, lines):
        small_copy(step - 1, (a + step) % lines, a).wait_send()
        count_copy(step - 1, (a + step) % lines, a).wait_send()
    for p in range(4):
        for which, line in enumerate((beside(a), above(a))):
            first_hop(p, a, line, which).wait_send()

    first_copy(t // 2).wait_send()

    def sent(s, _):
        home_sent(out_home, s)
        home_sent(grad_home, s)

        @pl.when(a != s)
        def _():
            norm_copy(s).wait_send()

        @pl.when(c == 0)
        def _():
            for j in streams:
                kv_copy(s, j).wait_send()

        @pl.when(c == 1)
        def _():
            dkv_copy(s).wait_send()

        for index in range(8):
            rows_sent(index, s)
        for p in range(4):

            @pl.when((a == beside(s)) | (a == above(s)))
            def _():
                second_hop(p, s, 0).wait_send()

            @pl.when(a != s)
            def _():
                core_hop(p, s, c).wait_send()

        return 0

    lax.fori_loop(0, lines, sent, 0)


def relay_call(inputs, cotangent, lengths, chosen, singles, weights):
    lines = lax.axis_size("section")
    chips = lax.axis_size("tensor")
    rows, buckets, width = inputs.shape[1:]
    local, total, half = rows * chips, 2 * rows * chips, width // 2
    head_width, units = weights["wo_in"].shape[0], weights["wp_in"].shape[0]
    heads = head_width // HDIM
    stream = local // STREAMS
    peers, owned = chips - 1, stream // 2
    vmem, dma = pltpu.VMEM, pltpu.SemaphoreType.DMA
    operands = dict(
        inputs=inputs,
        cotangent=cotangent,
        lengths=lengths,
        chosen=chosen,
        **singles,
        **weights,
    )

    def space(name):
        if name in weights:
            return pl.ANY
        return pltpu.SMEM if operands[name] is lengths else pltpu.VMEM

    sums = dict(
        acts=((lines, rows, width), LOW),
        grads=((lines, rows, width), LOW),
        ends=((2 * chips, 8, width), F32),
    )
    gathered = dict(
        all_nrm=((lines, 2, STREAMS, stream, half), LOW),
        all_nmlp=((lines, 2, STREAMS, stream, half), LOW),
        all_ups=((lines, 2, STREAMS, stream, half), LOW),
        all_brn=((lines, 2, STREAMS, stream, half), LOW),
        all_act=((lines, 2, STREAMS, stream, units), LOW),
        all_gpre=((lines, 2, STREAMS, stream, units), LOW),
        all_mix=((lines, 2, STREAMS, stream, head_width), LOW),
        all_dqkv=((lines, 2, 3, STREAMS, stream, head_width), LOW),
    )
    outputs = dict(**sums, **gathered)
    scratch = dict(
        wq=vmem((lines,) + weights["wq_in"].shape, LOW),
        wo=vmem((lines,) + weights["wo_in"].shape, LOW),
        wf=vmem((lines,) + weights["wf_in"].shape, LOW),
        wp=vmem((lines,) + weights["wp_in"].shape, LOW),
        small_own=vmem((8, width), F32),
        small=vmem((lines, 8, width), F32),
        count_own=vmem((lines, 8, total), F32),
        count=vmem((lines, 8, total), F32),
        hidden=vmem((STREAMS, owned, width), F32),
        middle=vmem((STREAMS, owned, width), F32),
        upstream=vmem((STREAMS, owned, width), LOW),
        first_out=vmem((2, owned, width), LOW),
        first_in=vmem((STREAMS, 2, owned, width), LOW),
        xhat1=vmem((lines, STREAMS, owned, width), F32),
        inv1=vmem((lines, STREAMS, owned, 128), F32),
        xhat2=vmem((lines, STREAMS, owned, width), F32),
        inv2=vmem((lines, STREAMS, owned, 128), F32),
        nrm=vmem((lines, STREAMS, stream, width), LOW),
        nmlp=vmem((lines, STREAMS, stream, width), LOW),
        ups=vmem((lines, STREAMS, stream, width), LOW),
        brn=vmem((lines, STREAMS, stream, width), LOW),
        act=vmem((lines, STREAMS, stream, units), LOW),
        gpre=vmem((lines, STREAMS, stream, units), LOW),
        slope=vmem((lines, STREAMS, stream, units), F32),
        mix=vmem((lines, STREAMS, stream, head_width), LOW),
        qry=vmem((lines, STREAMS, stream, head_width), LOW),
        gmix=vmem((STREAMS, stream, head_width), LOW),
        dqkv=vmem((lines, 3, STREAMS, stream, head_width), LOW),
        pass_ups=vmem((STREAMS, stream, width), LOW),
        pass_gpre=vmem((STREAMS, stream, units), LOW),
        kv=vmem((lines, 2, total, head_width), LOW),
        soft=vmem((lines, STREAMS, heads, stream, total), F32),
        near=vmem((STREAMS, stream, total), F32),
        dkv_all=vmem((2, total, head_width), F32),
        dkv_out=vmem((lines, 2, local, head_width), LOW),
        dkv_in=vmem((lines, 2, local, head_width), LOW),
        part=vmem((4, STREAMS, stream, width), LOW),
        arrived=vmem((lines, 4, STREAMS, peers, owned, width), LOW),
        out_low=vmem((lines, STREAMS, owned, width), LOW),
        grad_low=vmem((lines, STREAMS, owned, width), LOW),
        norm_part=vmem((lines, 8, width), F32),
        norm_all=vmem((lines, 8, width), F32),
        w_first_s=dma((4, 2)),
        w_first_r=dma((lines, 4)),
        w_second_s=dma((lines, 4)),
        w_second_r=dma((lines, 4, 2)),
        w_core_s=dma((lines, 4)),
        w_core_r=dma((lines, 4)),
        w_own=dma((4,)),
        small_s=dma((lines - 1,)),
        small_r=dma((lines,)),
        count_s=dma((lines - 1,)),
        count_r=dma((lines,)),
        ag_s=dma((4, STREAMS, peers)),
        ag_r=dma((4, STREAMS, peers)),
        rs_s=dma((4, STREAMS, peers)),
        rs_r=dma((4, STREAMS, peers)),
        kv_s=dma((lines, STREAMS)),
        kv_r=dma((lines, STREAMS)),
        dkv_s=dma((lines,)),
        dkv_r=dma((lines,)),
        rows_s=dma((8, lines, 2)),
        rows_r=dma((8,)),
        pass_s=dma((2,)),
        pass_r=dma((2,)),
        pass_on_s=dma((2, 2)),
        share_s=dma((4,)),
        share_r=dma((4,)),
        heads_r=dma((lines,)),
        heads_s=dma((lines,)),
        heads_sr=dma((lines,)),
        first_s=dma,
        first_r=dma((STREAMS,)),
        out_s=dma((lines, STREAMS)),
        out_r=dma,
        grad_s=dma((lines, STREAMS)),
        grad_r=dma,
        norm_s=dma((lines,)),
        norm_r=dma,
        ends_s=dma((2 * chips - 1,)),
        ends_r=dma,
    )
    names = tuple(operands) + tuple(outputs) + tuple(scratch)
    results = pl.pallas_call(
        functools.partial(relay_kernel, names),
        out_shape=[jax.ShapeDtypeStruct(shape, kind) for shape, kind in outputs.values()],
        in_specs=[pl.BlockSpec(memory_space=space(name)) for name in operands],
        out_specs=[
            pl.BlockSpec(memory_space=pl.ANY if name in gathered else pltpu.VMEM)
            for name in outputs
        ],
        scratch_shapes=list(scratch.values()),
        compiler_params=pltpu.CompilerParams(
            collective_id=0, has_side_effects=True, vmem_limit_bytes=60 * 2**20
        ),
        name="relay",
    )(*operands.values())
    return dict(zip(outputs, results))


def weights_kernel(names, *refs):
    r = types.SimpleNamespace(**dict(zip(names, refs)))
    micro_count, rows, buckets, width = r.activations.shape
    chips, units, head_width = r.ends.shape[0] // 2, r.all_act.shape[-1], r.all_mix.shape[-1]
    lines = r.acts.shape[0]
    loads = [
        pltpu.make_async_copy(source, target, r.load_sem.at[place])
        for place, (source, target) in enumerate(
            (
                (r.all_act, r.act),
                (r.all_ups, r.ups),
                (r.all_nmlp, r.nmlp),
                (r.all_gpre, r.gpre),
                (r.all_mix, r.mix),
                (r.all_brn, r.brn),
                (r.all_nrm, r.nrm),
                (r.all_dqkv, r.dqkv),
            )
        )
    ]
    stores = [
        pltpu.make_async_copy(source, target, r.store_sem.at[place])
        for place, (source, target) in enumerate(
            (
                (r.own_proj, r.w_proj),
                (r.own_fc, r.w_fc),
                (r.own_out, r.w_out),
                (r.own_qkv, r.w_qkv),
            )
        )
    ]
    for load in loads:
        load.start()

    sums = r.ends[0]
    for other in range(1, 2 * chips):
        sums = sums + r.ends[other]
    singles = (r.ln1_gain, r.ln1_shift, r.ln2_gain, r.ln2_shift, r.b_out, r.b_proj)
    for place, single in enumerate(singles):
        single[...] = sums[place : place + 1]
    for chip in range(chips):
        both = r.ends[chip] + r.ends[chips + chip]
        r.b_fc[:, chip * units : (chip + 1) * units] = both[6:7, :units]
        here = slice(chip * head_width, (chip + 1) * head_width)
        r.b_qv[0:1, here] = both[7:8, :head_width]
        r.b_qv[1:2, here] = both[7:8, width // 2 : width // 2 + head_width]
    for target, source in ((r.activations, r.acts), (r.in_grads, r.grads)):
        for micro in range(micro_count):
            rows_of = [
                source[micro * buckets + bucket].astype(F32)[:, None, :]
                for bucket in range(buckets)
            ]
            target[micro] = jnp.concatenate(rows_of, axis=1).astype(LOW)

    def flat(array):
        return array.reshape(lines * 2 * chips * rows, array.shape[-1])

    loads[0].wait()
    loads[1].wait()
    r.own_proj[...] = dot_tn(flat(r.act[...]), flat(r.ups[...]))
    stores[0].start()
    loads[2].wait()
    loads[3].wait()
    r.own_fc[...] = dot_tn(flat(r.nmlp[...]), flat(r.gpre[...]))
    stores[1].start()
    loads[4].wait()
    loads[5].wait()
    r.own_out[...] = dot_tn(flat(r.mix[...]), flat(r.brn[...]))
    stores[2].start()
    loads[6].wait()
    loads[7].wait()
    nrm = flat(r.nrm[...])
    for which in range(3):
        r.own_qkv[which] = dot_tn(flat(r.dqkv[:, :, which]), nrm)
    stores[3].start()
    for store in stores:
        store.wait()


def weights_call(relayed, inputs_shape, head_width, units):
    chips = lax.axis_size("tensor")
    width = inputs_shape[-1]
    half = width // 2
    outputs = dict(
        activations=(inputs_shape, LOW),
        in_grads=(inputs_shape, LOW),
        ln1_gain=((1, width), F32),
        ln1_shift=((1, width), F32),
        w_qkv=((3, head_width, half), F32),
        b_qv=((2, width), F32),
        w_out=((head_width, half), F32),
        b_out=((1, width), F32),
        ln2_gain=((1, width), F32),
        ln2_shift=((1, width), F32),
        w_fc=((half, units), F32),
        b_fc=((1, chips * units), F32),
        w_proj=((units, half), F32),
        b_proj=((1, width), F32),
    )
    rows = ("act", "ups", "nmlp", "gpre", "mix", "brn", "nrm", "dqkv")
    own = dict(own_proj="w_proj", own_fc="w_fc", own_out="w_out", own_qkv="w_qkv")
    scratch = {name: pltpu.VMEM(relayed["all_" + name].shape, LOW) for name in rows}
    scratch.update({name: pltpu.VMEM(outputs[of][0], F32) for name, of in own.items()})
    scratch["load_sem"] = pltpu.SemaphoreType.DMA((8,))
    scratch["store_sem"] = pltpu.SemaphoreType.DMA((4,))
    whole, apart = pl.BlockSpec(memory_space=pltpu.VMEM), pl.BlockSpec(memory_space=pl.ANY)
    small = ("acts", "grads", "ends")
    return pl.pallas_call(
        functools.partial(weights_kernel, tuple(relayed) + tuple(outputs) + tuple(scratch)),
        out_shape=[jax.ShapeDtypeStruct(shape, kind) for shape, kind in outputs.values()],
        in_specs=[whole if name in small else apart for name in relayed],
        out_specs=[apart if name in own.values() else whole for name in outputs],
        scratch_shapes=list(scratch.values()),
        compiler_params=pltpu.CompilerParams(vmem_limit_bytes=60 * 2**20),
        name="weight_gradients",
    )(*relayed.values())


def on_line(
    inputs,
    cotangent,
    lengths,
    chosen,
    ln1_gain,
    ln1_shift,
    w_qkv,
    b_qv,
    w_out,
    b_out,
    ln2_gain,
    ln2_shift,
    w_fc,
    b_fc,
    w_proj,
    b_proj,
):
    head_width, units = w_out.shape[1], w_fc.shape[2]
    singles = dict(
        ln1_gain=ln1_gain,
        ln1_shift=ln1_shift,
        ln2_gain=ln2_gain,
        ln2_shift=ln2_shift,
        b_out=b_out,
        b_proj=b_proj,
        b_fc=b_fc,
        b_qv=b_qv[0],
    )
    weights = dict(
        wq_in=jnp.swapaxes(w_qkv[0], 1, 2).reshape(-1, inputs.shape[-1]),
        wo_in=w_out[0],
        wf_in=w_fc[0],
        wp_in=w_proj[0],
    )
    picks = chosen.reshape((-1,) + chosen.shape[-2:])
    relayed = relay_call(inputs, cotangent, lengths, picks, singles, weights)
    results = list(weights_call(relayed, inputs.shape, head_width, units))
    results[4] = jnp.swapaxes(results[4], 1, 2)
    vectors = (2, 3, 7, 8, 9, 11, 13)
    return tuple(
        result if place in vectors else result[None] for place, result in enumerate(results)
    )


def fits_lines(mesh):
    return mesh.shape["section"] == 4 and mesh.shape["seq"] == 2 and mesh.shape["tensor"] == 4


def solution(mesh):
    placed = (
        P(None, ("seq", "tensor"), None, None),
        P(None, ("seq", "tensor"), None, None),
        P(),
        P("section", None, None, "tensor", "seq", None),
        P("section", None),
        P("section", None),
        P("section", None, None, "tensor"),
        P("section", None, "tensor"),
        P("section", "tensor", None),
        P("section", None),
        P("section", None),
        P("section", None),
        P("section", None, "tensor"),
        P("section", "tensor"),
        P("section", "tensor", None),
        P("section", None),
    )
    return jax.shard_map(
        on_line if fits_lines(mesh) else on_device,
        mesh=mesh,
        in_specs=placed,
        out_specs=(
            P("section", None, ("seq", "tensor"), None, None),
            P("section", None, ("seq", "tensor"), None, None),
            P("section", None),
            P("section", None),
            P("section", None, "seq", "tensor"),
            P("section", None, None),
            P("section", "tensor", "seq"),
            P("section", None),
            P("section", None),
            P("section", None),
            P("section", "seq", "tensor"),
            P("section", None),
            P("section", "tensor", "seq"),
            P("section", None),
        ),
        check_vma=False,
    )
```

```python
import functools
import types

import jax
import jax.numpy as jnp
from jax import lax
from jax.experimental import pallas as pl
from jax.experimental.pallas import tpu as pltpu
from jax.sharding import PartitionSpec as P

HDIM = 64
WIN = 64
QB = 64
KSEL = 64


NORM_EPS = 1e-05
MASKED = -1000000000.0


def from_behind(value, axis, steps):
    count = lax.axis_size(axis)
    first, last = (max(0, -steps), min(count, count - steps))
    return lax.ppermute(value, axis, [(source, source + steps) for source in range(first, last)])


def layer_norm(values, gain, shift):
    average = jnp.mean(values, axis=-1, keepdims=True)
    centred = values - average
    variance = jnp.mean(centred * centred, axis=-1, keepdims=True)
    return centred * lax.rsqrt(variance + NORM_EPS) * gain + shift


def gelu_tanh(values):
    return (
        0.5
        * values
        * (1.0 + jnp.tanh(0.7978845608028654 * (values + 0.044715 * values * values * values)))
    )


def gather_rows(row_block):
    return lax.all_gather(row_block, "tensor", axis=0, tiled=True)


def scatter_product(left_rows, weight, formula):
    return lax.psum_scatter(
        jnp.einsum(formula, left_rows, weight, preferred_element_type=jnp.float32).astype(
            jnp.bfloat16
        ),
        "tensor",
        scatter_dimension=0,
        tiled=True,
    ).astype(jnp.float32)


def near_slabs(full_rows, seq_start, seq_first, length_local):
    buckets = full_rows.shape[1]
    heads_local = full_rows.shape[2] // HDIM
    blocks = length_local // QB
    earlier = lax.dynamic_slice_in_dim(full_rows, jnp.maximum(seq_start - WIN, 0), WIN, 0)
    earlier = jnp.where(seq_first, jnp.zeros_like(earlier), earlier)
    local_part = lax.dynamic_slice_in_dim(full_rows, seq_start, length_local, 0)
    segment = jnp.concatenate([earlier, local_part], 0).reshape(
        length_local + WIN, buckets, heads_local, HDIM
    )
    return jnp.concatenate(
        [
            segment[offset_index * QB : offset_index * QB + length_local].reshape(
                blocks, QB, buckets, heads_local, HDIM
            )
            for offset_index in range(WIN // QB + 1)
        ],
        1,
    )


def far_rows(full_rows, flat_index):
    total_rows, buckets, feature_width = full_rows.shape
    heads_local = feature_width // HDIM
    return jnp.take(full_rows.reshape(total_rows * buckets * heads_local, HDIM), flat_index, axis=0)


def key_geometry(chosen_now, seq_start, blocks):
    buckets, heads_local = (chosen_now.shape[0], chosen_now.shape[1])
    bucket_ids = lax.broadcasted_iota(jnp.int32, chosen_now.shape, 0)
    head_ids = lax.broadcasted_iota(jnp.int32, chosen_now.shape, 1)
    flat_index = (chosen_now * buckets + bucket_ids) * heads_local + head_ids
    block_start = seq_start + QB * lax.broadcasted_iota(jnp.int32, (blocks, 1, 1), 0)
    query_ids = lax.broadcasted_iota(jnp.int32, (1, QB, 1), 1)
    key_ids = lax.broadcasted_iota(jnp.int32, (1, 1, WIN + QB), 2)
    distance = query_ids + WIN - key_ids
    near_ok = (distance >= 0) & (distance < WIN) & (block_start + key_ids - WIN >= 0)
    far_ok = chosen_now + WIN <= block_start.reshape(1, 1, blocks, 1)
    near_mask = jnp.broadcast_to(
        near_ok[:, None, None], (blocks, buckets, heads_local, QB, WIN + QB)
    )
    far_mask = jnp.broadcast_to(
        jnp.transpose(far_ok, (2, 0, 1, 3))[:, :, :, None, :],
        (blocks, buckets, heads_local, QB, KSEL),
    )
    return (flat_index, jnp.concatenate([near_mask, far_mask], -1))


def attention_setup(queries, key_rows, value_rows, chosen_now, seq_start, seq_first):
    length_local, buckets, feature_width = queries.shape
    heads_local = feature_width // HDIM
    blocks = length_local // QB
    query_blocks = queries.reshape(blocks, QB, buckets, heads_local, HDIM)
    flat_index, key_mask = key_geometry(chosen_now, seq_start, blocks)
    near_keys = near_slabs(key_rows, seq_start, seq_first, length_local)
    near_values = near_slabs(value_rows, seq_start, seq_first, length_local)
    far_keys = far_rows(key_rows, flat_index)
    far_values = far_rows(value_rows, flat_index)
    near_scores = jnp.einsum(
        "bqnhe,btnhe->bnhqt", query_blocks, near_keys, preferred_element_type=jnp.float32
    )
    far_scores = jnp.einsum(
        "bqnhe,nhbke->bnhqk", query_blocks, far_keys, preferred_element_type=jnp.float32
    )
    scores = jnp.where(
        key_mask, HDIM ** (-0.5) * jnp.concatenate([near_scores, far_scores], -1), MASKED
    )
    return (query_blocks, near_keys, near_values, far_keys, far_values, flat_index, scores)


def attend(queries, key_rows, value_rows, chosen_now, seq_start, seq_first):
    query_blocks, near_keys, near_values, far_keys, far_values, flat_index, scores = (
        attention_setup(queries, key_rows, value_rows, chosen_now, seq_start, seq_first)
    )
    span = WIN + QB
    row_top = jnp.max(scores, -1, keepdims=True)
    exp_terms = jnp.exp(scores - row_top)
    row_total = jnp.sum(exp_terms, -1, keepdims=True)
    softmax_low = (exp_terms / row_total).astype(jnp.bfloat16)
    near_part = jnp.einsum(
        "bnhqt,btnhe->bqnhe",
        softmax_low[..., :span],
        near_values,
        preferred_element_type=jnp.float32,
    )
    far_part = jnp.einsum(
        "bnhqk,nhbke->bqnhe",
        softmax_low[..., span:],
        far_values,
        preferred_element_type=jnp.float32,
    )
    return ((near_part + far_part).reshape(queries.shape), row_top + jnp.log(row_total))


def spread_back(near_grad, far_grad, flat_index, seq_start, seq_first, total_rows):
    blocks, span, buckets, heads_local, head_size = near_grad.shape
    length_local = blocks * QB
    feature_width = heads_local * head_size
    segment = jnp.zeros((length_local + WIN, buckets, heads_local, head_size), jnp.float32)
    for offset_index in range(WIN // QB + 1):
        piece = near_grad[:, offset_index * QB : (offset_index + 1) * QB].reshape(
            length_local, buckets, heads_local, head_size
        )
        segment = segment.at[offset_index * QB : offset_index * QB + length_local].add(piece)
    full_rows = jnp.zeros((total_rows * buckets * heads_local, head_size), jnp.float32)
    full_rows = full_rows.at[flat_index.reshape(-1)].add(far_grad.reshape(-1, head_size))
    full_rows = full_rows.reshape(total_rows, buckets, feature_width)
    local_part = segment[WIN:].reshape(length_local, buckets, feature_width)
    earlier = jnp.where(seq_first, 0.0, segment[:WIN].reshape(WIN, buckets, feature_width))
    full_rows = lax.dynamic_update_slice_in_dim(
        full_rows,
        lax.dynamic_slice_in_dim(full_rows, seq_start, length_local, 0) + local_part,
        seq_start,
        0,
    )
    earlier_start = jnp.maximum(seq_start - WIN, 0)
    full_rows = lax.dynamic_update_slice_in_dim(
        full_rows,
        lax.dynamic_slice_in_dim(full_rows, earlier_start, WIN, 0) + earlier,
        earlier_start,
        0,
    )
    return full_rows


def attend_back(
    queries, key_rows, value_rows, chosen_now, seq_start, seq_first, log_total, grad_mixed
):
    query_blocks, near_keys, near_values, far_keys, far_values, flat_index, scores = (
        attention_setup(queries, key_rows, value_rows, chosen_now, seq_start, seq_first)
    )
    span = WIN + QB
    score_scale = HDIM ** (-0.5)
    grad_blocks = grad_mixed.reshape(query_blocks.shape)
    weights_full = jnp.exp(scores - log_total)
    softmax_low = weights_full.astype(jnp.bfloat16)
    grad_near_weights = jnp.einsum(
        "bqnhe,btnhe->bnhqt", grad_blocks, near_values, preferred_element_type=jnp.float32
    )
    grad_far_weights = jnp.einsum(
        "bqnhe,nhbke->bnhqk", grad_blocks, far_values, preferred_element_type=jnp.float32
    )
    grad_weights = jnp.concatenate([grad_near_weights, grad_far_weights], -1)
    row_dot = jnp.sum(weights_full * grad_weights, -1, keepdims=True)
    grad_scores = (weights_full * (grad_weights - row_dot)).astype(jnp.bfloat16)
    grad_near, grad_far = (grad_scores[..., :span], grad_scores[..., span:])
    grad_queries = score_scale * (
        jnp.einsum("bnhqt,btnhe->bqnhe", grad_near, near_keys, preferred_element_type=jnp.float32)
        + jnp.einsum("bnhqk,nhbke->bqnhe", grad_far, far_keys, preferred_element_type=jnp.float32)
    )
    near_key_grad = score_scale * jnp.einsum(
        "bnhqt,bqnhe->btnhe", grad_near, query_blocks, preferred_element_type=jnp.float32
    )
    far_key_grad = score_scale * jnp.einsum(
        "bnhqk,bqnhe->nhbke", grad_far, query_blocks, preferred_element_type=jnp.float32
    )
    near_value_grad = jnp.einsum(
        "bnhqt,bqnhe->btnhe",
        softmax_low[..., :span],
        grad_blocks,
        preferred_element_type=jnp.float32,
    )
    far_value_grad = jnp.einsum(
        "bnhqk,bqnhe->nhbke",
        softmax_low[..., span:],
        grad_blocks,
        preferred_element_type=jnp.float32,
    )
    total_rows = key_rows.shape[0]
    key_grad = spread_back(
        near_key_grad, far_key_grad, flat_index, seq_start, seq_first, total_rows
    )
    value_grad = spread_back(
        near_value_grad, far_value_grad, flat_index, seq_start, seq_first, total_rows
    )
    return (grad_queries.reshape(queries.shape), key_grad, value_grad)


def forward_pass(hidden, params, chosen_now, query_mask, seq_start, seq_first, finish):
    (
        ln1_gain,
        ln1_shift,
        w_qkv,
        b_qv,
        w_out,
        b_out,
        ln2_gain,
        ln2_shift,
        w_fc,
        b_fc,
        w_proj,
        b_proj,
    ) = params
    hidden_wide = hidden.astype(jnp.float32)
    normed_all = gather_rows(layer_norm(hidden_wide, ln1_gain, ln1_shift).astype(jnp.bfloat16))
    projected = jnp.einsum("pnd,jdc->jpnc", normed_all, w_qkv, preferred_element_type=jnp.float32)
    queries = (projected[0] + b_qv[0]).astype(jnp.bfloat16)
    key_rows, value_rows = (
        lax.all_gather(projected[1].astype(jnp.bfloat16), "seq", axis=0, tiled=True),
        lax.all_gather((projected[2] + b_qv[1]).astype(jnp.bfloat16), "seq", axis=0, tiled=True),
    )
    attended, log_total = attend(queries, key_rows, value_rows, chosen_now, seq_start, seq_first)
    mixed_rows = (attended * query_mask[:, :, None]).astype(jnp.bfloat16)
    middle = hidden_wide + scatter_product(mixed_rows, w_out, "pnc,cd->pnd") + b_out
    normed_mlp = gather_rows(layer_norm(middle, ln2_gain, ln2_shift).astype(jnp.bfloat16))
    pre_active = (
        jnp.einsum("pnd,df->pnf", normed_mlp, w_fc, preferred_element_type=jnp.float32) + b_fc
    )
    active = gelu_tanh(pre_active).astype(jnp.bfloat16)
    if not finish:
        return (
            normed_all,
            queries,
            key_rows,
            value_rows,
            log_total,
            mixed_rows,
            middle,
            normed_mlp,
            pre_active,
            active,
        )
    output = (middle + scatter_product(active, w_proj, "pnf,fd->pnd") + b_proj).astype(jnp.bfloat16)
    return (output, (key_rows, value_rows))


def backward_pass(hidden, upstream, params, chosen_now, query_mask, seq_start, seq_first):
    (
        ln1_gain,
        ln1_shift,
        w_qkv,
        b_qv,
        w_out,
        b_out,
        ln2_gain,
        ln2_shift,
        w_fc,
        b_fc,
        w_proj,
        b_proj,
    ) = params
    (
        normed_all,
        queries,
        key_rows,
        value_rows,
        log_total,
        mixed_rows,
        middle,
        normed_mlp,
        pre_active,
        active,
    ) = forward_pass(hidden, params, chosen_now, query_mask, seq_start, seq_first, False)
    upstream_all = gather_rows(upstream)
    grad_w_proj = jnp.einsum(
        "pnf,pnd->fd", active, upstream_all, preferred_element_type=jnp.float32
    )
    grad_b_proj = jnp.sum(upstream.astype(jnp.float32), axis=(0, 1))
    grad_active = jnp.einsum(
        "pnd,fd->pnf", upstream_all, w_proj, preferred_element_type=jnp.float32
    )
    unused_value, gelu_pull = jax.vjp(gelu_tanh, pre_active)
    grad_pre = gelu_pull(grad_active)[0].astype(jnp.bfloat16)
    grad_w_fc = jnp.einsum("pnd,pnf->df", normed_mlp, grad_pre, preferred_element_type=jnp.float32)
    grad_b_fc = jnp.sum(grad_pre.astype(jnp.float32), axis=(0, 1))
    grad_normed_mlp = scatter_product(grad_pre, w_fc, "pnf,df->pnd")
    unused_norm, second_pull = jax.vjp(layer_norm, middle, ln2_gain, ln2_shift)
    grad_mid_norm, grad_ln2_gain, grad_ln2_shift = second_pull(grad_normed_mlp)
    grad_middle = upstream.astype(jnp.float32) + grad_mid_norm
    grad_branch = grad_middle.astype(jnp.bfloat16)
    grad_b_out = jnp.sum(grad_branch.astype(jnp.float32), axis=(0, 1))
    branch_all = gather_rows(grad_branch)
    grad_w_out = jnp.einsum(
        "pnc,pnd->cd", mixed_rows, branch_all, preferred_element_type=jnp.float32
    )
    grad_mixed = jnp.einsum(
        "pnd,cd->pnc", branch_all, w_out, preferred_element_type=jnp.float32
    ).astype(jnp.bfloat16) * query_mask[:, :, None].astype(jnp.bfloat16)
    grad_queries, key_grad_all, value_grad_all = attend_back(
        queries, key_rows, value_rows, chosen_now, seq_start, seq_first, log_total, grad_mixed
    )
    key_grad, value_grad = (
        lax.psum_scatter(
            key_grad_all.astype(jnp.bfloat16), "seq", scatter_dimension=0, tiled=True
        ).astype(jnp.float32),
        lax.psum_scatter(
            value_grad_all.astype(jnp.bfloat16), "seq", scatter_dimension=0, tiled=True
        ).astype(jnp.float32),
    )
    grad_project = jnp.stack(
        [
            grad_queries.astype(jnp.bfloat16),
            key_grad.astype(jnp.bfloat16),
            value_grad.astype(jnp.bfloat16),
        ],
        2,
    )
    grad_w_qkv = jnp.einsum(
        "pnd,pnjc->jdc", normed_all, grad_project, preferred_element_type=jnp.float32
    )
    grad_b_qv = jnp.sum(grad_project[:, :, 0::2].astype(jnp.float32), axis=(0, 1))
    grad_normed = scatter_product(grad_project, w_qkv, "pnjc,jdc->pnd")
    unused_first, first_pull = jax.vjp(layer_norm, hidden.astype(jnp.float32), ln1_gain, ln1_shift)
    grad_in_norm, grad_ln1_gain, grad_ln1_shift = first_pull(grad_normed)
    grad_hidden = (grad_middle + grad_in_norm).astype(jnp.bfloat16)
    block_grads = (
        grad_ln1_gain,
        grad_ln1_shift,
        grad_w_qkv,
        grad_b_qv,
        grad_w_out,
        grad_b_out,
        grad_ln2_gain,
        grad_ln2_shift,
        grad_w_fc,
        grad_b_fc,
        grad_w_proj,
        grad_b_proj,
    )
    return (grad_hidden, block_grads)


def on_device(
    inputs,
    cotangent,
    lengths,
    chosen,
    ln1_gain,
    ln1_shift,
    w_qkv,
    b_qv,
    w_out,
    b_out,
    ln2_gain,
    ln2_shift,
    w_fc,
    b_fc,
    w_proj,
    b_proj,
):
    params = tuple(
        (
            weight_array[0]
            for weight_array in (
                ln1_gain,
                ln1_shift,
                w_qkv,
                b_qv,
                w_out,
                b_out,
                ln2_gain,
                ln2_shift,
                w_fc,
                b_fc,
                w_proj,
                b_proj,
            )
        )
    )
    section_index = lax.axis_index("section")
    section_count = lax.axis_size("section")
    seq_index = lax.axis_index("seq")
    tensor_index = lax.axis_index("tensor")
    tensor_count = lax.axis_size("tensor")
    micro_count, rows_local, buckets, feature_width = inputs.shape
    length_local = rows_local * tensor_count
    heads_width = w_qkv.shape[-1]
    seq_start = seq_index * length_local
    seq_first = seq_index == 0
    positions = seq_start + lax.broadcasted_iota(jnp.int32, (micro_count, length_local, buckets), 1)
    mask_all = (positions < lengths[:, None, :]).astype(jnp.float32)
    mask_rows = lax.dynamic_slice_in_dim(mask_all, tensor_index * rows_local, rows_local, 1)
    step_count = micro_count + section_count - 1
    chosen_section = chosen[0]
    received = jnp.zeros((rows_local, buckets, feature_width), jnp.bfloat16)
    stored = jnp.zeros((micro_count, rows_local, buckets, feature_width), jnp.bfloat16)
    outputs = jnp.zeros_like(stored)
    for step_index in range(step_count):
        micro_index = step_index - section_index
        running = (micro_index >= 0) & (micro_index < micro_count)
        slot_index = jnp.clip(micro_index, 0, micro_count - 1)
        block_in = jnp.where(
            section_index == 0, lax.dynamic_index_in_dim(inputs, slot_index, 0, False), received
        )
        chosen_now = lax.dynamic_index_in_dim(chosen_section, slot_index, 0, False)
        query_mask = lax.dynamic_index_in_dim(mask_all, slot_index, 0, False)
        result, key_pair = forward_pass(
            block_in, params, chosen_now, query_mask, seq_start, seq_first, True
        )
        stored = jnp.where(
            running, lax.dynamic_update_index_in_dim(stored, block_in, slot_index, 0), stored
        )
        outputs = jnp.where(
            running, lax.dynamic_update_index_in_dim(outputs, result, slot_index, 0), outputs
        )
        received = from_behind(result, "section", 1)
    back_received = jnp.zeros((rows_local, buckets, feature_width), jnp.bfloat16)
    in_grads = jnp.zeros_like(stored)
    totals = None
    for step_index in range(step_count):
        micro_index = step_index - (section_count - 1 - section_index)
        running = (micro_index >= 0) & (micro_index < micro_count)
        slot_index = jnp.clip(micro_index, 0, micro_count - 1)
        chosen_now = lax.dynamic_index_in_dim(chosen_section, slot_index, 0, False)
        query_mask = lax.dynamic_index_in_dim(mask_all, slot_index, 0, False)
        local_mask = lax.dynamic_index_in_dim(mask_rows, slot_index, 0, False)
        top_grad = (
            lax.dynamic_index_in_dim(cotangent, slot_index, 0, False).astype(jnp.float32)
            * local_mask[:, :, None]
        ).astype(jnp.bfloat16)
        upstream = jnp.where(section_index == section_count - 1, top_grad, back_received)
        hidden = lax.dynamic_index_in_dim(stored, slot_index, 0, False)
        grad_hidden, block_grads = backward_pass(
            hidden, upstream, params, chosen_now, query_mask, seq_start, seq_first
        )
        block_grads = tuple(
            (jnp.where(running, grad_part, jnp.zeros_like(grad_part)) for grad_part in block_grads)
        )
        totals = (
            block_grads
            if step_index == 0
            else tuple(
                (total_part + grad_part for total_part, grad_part in zip(totals, block_grads))
            )
        )
        in_grads = jnp.where(
            running, lax.dynamic_update_index_in_dim(in_grads, grad_hidden, slot_index, 0), in_grads
        )
        back_received = from_behind(grad_hidden, "section", -1)
    (
        sum_ln1_gain,
        sum_ln1_shift,
        sum_w_qkv,
        sum_b_qv,
        sum_w_out,
        sum_b_out,
        sum_ln2_gain,
        sum_ln2_shift,
        sum_w_fc,
        sum_b_fc,
        sum_w_proj,
        sum_b_proj,
    ) = totals
    part_qkv, part_out, part_fc, part_proj = (
        lax.psum_scatter(
            sum_w_qkv.astype(jnp.bfloat16), "seq", scatter_dimension=1, tiled=True
        ).astype(jnp.float32),
        lax.psum_scatter(
            sum_w_out.astype(jnp.bfloat16), "seq", scatter_dimension=1, tiled=True
        ).astype(jnp.float32),
        lax.psum_scatter(
            sum_w_fc.astype(jnp.bfloat16), "seq", scatter_dimension=0, tiled=True
        ).astype(jnp.float32),
        lax.psum_scatter(
            sum_w_proj.astype(jnp.bfloat16), "seq", scatter_dimension=1, tiled=True
        ).astype(jnp.float32),
    )
    bias_qv = lax.dynamic_update_slice_in_dim(
        jnp.zeros((2, feature_width), jnp.float32), sum_b_qv, tensor_index * heads_width, 1
    )
    units_local = sum_b_fc.shape[0]
    bias_fc = lax.dynamic_update_slice_in_dim(
        jnp.zeros((units_local * tensor_count,), jnp.float32),
        sum_b_fc,
        tensor_index * units_local,
        0,
    )
    small_sums = lax.psum(
        (
            sum_ln1_gain,
            sum_ln1_shift,
            bias_qv,
            sum_b_out,
            sum_ln2_gain,
            sum_ln2_shift,
            bias_fc,
            sum_b_proj,
        ),
        ("seq", "tensor"),
    )
    return (
        outputs[None],
        in_grads[None],
        small_sums[0][None],
        small_sums[1][None],
        part_qkv[None],
        small_sums[2][None],
        part_out[None],
        small_sums[3][None],
        small_sums[4][None],
        small_sums[5][None],
        part_fc[None],
        small_sums[6][None],
        part_proj[None],
        small_sums[7][None],
    )


STREAMS = 2
NRM, NMLP, UPS, BRN, ACT, GPRE, MIX, DQKV = range(8)
F32 = jnp.float32
LOW = jnp.bfloat16
MESH_ID = pl.DeviceIdType.MESH


def dot_nn(left, right):
    return lax.dot_general(left, right, (((1,), (0,)), ((), ())), preferred_element_type=F32)


def dot_nt(left, right):
    return lax.dot_general(left, right, (((1,), (1,)), ((), ())), preferred_element_type=F32)


def dot_tn(left, right):
    return lax.dot_general(left, right, (((0,), (0,)), ((), ())), preferred_element_type=F32)


def standard(rows):
    centred = rows - jnp.mean(rows, axis=-1, keepdims=True)
    scale = lax.rsqrt(jnp.mean(centred * centred, axis=-1, keepdims=True) + NORM_EPS)
    return centred * scale, scale


def standard_back(grad, xhat, scale):
    inner = jnp.mean(grad * xhat, axis=-1, keepdims=True)
    return scale * (grad - jnp.mean(grad, axis=-1, keepdims=True) - xhat * inner)


def column_sum(rows):
    return jnp.sum(rows.astype(F32), axis=0, keepdims=True)


def relay_kernel(names, *refs):
    r = types.SimpleNamespace(**dict(zip(names, refs)))
    a, c, t = (lax.axis_index(name) for name in ("section", "seq", "tensor"))
    lines = lax.axis_size("section")
    chips = lax.axis_size("tensor")
    rows, buckets, width = r.inputs.shape[1:]
    half_width = width // 2
    local = rows * chips
    total = 2 * local
    stream_rows = local // STREAMS
    head_width = r.wo_in.shape[0]
    heads = head_width // HDIM
    blocks = local // QB
    units = r.wp_in.shape[0]
    scale = HDIM ** (-0.5)
    streams = range(STREAMS)

    def remote(src, dst, send, recv, **target):
        return pltpu.make_async_remote_copy(
            src_ref=src,
            dst_ref=dst,
            send_sem=send,
            recv_sem=recv,
            device_id=target,
            device_id_type=MESH_ID,
        )

    def drain(ref, sem):
        pltpu.make_async_copy(ref, ref, sem).wait()

    def row_block(index, size):
        return pl.ds(pl.multiple_of(index * size, size), size)

    near_chip = t + 1 - 2 * (t % 2)
    over_chip = (t + 2) % 4
    across_chip = 3 - t
    middle_chip = (t == 1) | (t == 2)
    end_chip = (t == 0) | (t == 3)
    owned = stream_rows // 2
    mine = row_block(t - 1, owned)
    my_half = row_block(c, local)

    r.kv[...] = jnp.zeros(r.kv.shape, LOW)

    barrier = pltpu.get_barrier_semaphore()
    greeted = 0
    for line in range(lines):
        for chip in range(chips):
            for core in range(2):
                if (line, chip, core) != (0, 0, 0) and (core == 0 or line * chip == 0):
                    there = {
                        "section": (a + line) % lines,
                        "seq": (c + core) % 2,
                        "tensor": (t + chip) % chips,
                    }
                    pl.semaphore_signal(barrier, inc=1, device_id=there, device_id_type=MESH_ID)
                    greeted += 1
    pl.semaphore_wait(barrier, greeted)

    def beside(s):
        return s + 1 - 2 * (s % 2)

    def above(s):
        return (s + 2) % 4

    def store(p):
        return (r.wq, r.wo, r.wf, r.wp)[p]

    def source(p):
        return (r.wq_in, r.wo_in, r.wf_in, r.wp_in)[p]

    def height(p):
        return source(p).shape[0]

    def core_half(p, s, core):
        return store(p).at[s, row_block(core, height(p) // 2)]

    def first_hop(p, s, neighbour, which):
        return remote(
            source(p).at[row_block(c, height(p) // 2)],
            core_half(p, s, c),
            r.w_first_s.at[p, which],
            r.w_first_r.at[s, p],
            section=neighbour,
        )

    def second_hop(p, s, which):
        view = store(p).at[s, row_block(2 * c + which, height(p) // 4)]
        return remote(
            view, view, r.w_second_s.at[s, p], r.w_second_r.at[s, p, which], section=3 - s
        )

    def core_hop(p, s, core):
        view = core_half(p, s, core)
        return remote(view, view, r.w_core_s.at[s, p], r.w_core_r.at[s, p], seq=1 - c)

    def own_copy(p):
        return pltpu.make_async_copy(source(p), store(p).at[a], r.w_own.at[p])

    def pass_on(s, p, which):
        line = (beside(s), above(s))[which]

        @pl.when(a == line)
        def _():
            first_hop(p, s, line, which).wait_recv()
            second_hop(p, s, which).start()
            core_hop(p, s, c).start()

    def pass_all(s, pieces):
        for p in pieces:
            for which in range(2):
                pass_on(s, p, which)

    def pass_far(s, p):
        @pl.when(a == 3 - s)
        def _():
            second_hop(p, s, 0).wait_recv()
            second_hop(p, s, 1).wait_recv()
            core_hop(p, s, c).start()

    def need(s, p):
        @pl.when(s == 0)
        def _():
            if p < 2:
                pass_all(0, (p,))
            pass_far(0, p)

        @pl.when(a == s)
        def _():
            own_copy(p).wait()

        @pl.when(a != s)
        def _():
            core_hop(p, s, 1 - c).wait_recv()

    def small_copy(step, line, slot):
        return remote(
            r.small_own, r.small.at[slot], r.small_s.at[step], r.small_r.at[slot], section=line
        )

    def count_copy(step, line, slot):
        return remote(
            r.count_own.at[line],
            r.count.at[slot],
            r.count_s.at[step],
            r.count_r.at[slot],
            section=line,
        )

    singles = (r.ln1_gain, r.ln1_shift, r.ln2_gain, r.ln2_shift, r.b_out, r.b_proj)
    for place, single in enumerate(singles):
        r.small_own[place : place + 1] = single[...]
    r.small_own[6:7, :units] = r.b_fc[...]
    r.small_own[7:8, :head_width] = r.b_qv[0:1]
    r.small_own[7:8, half_width : half_width + head_width] = r.b_qv[1:2]
    for step in range(1, lines):
        small_copy(step - 1, (a + step) % lines, a).start()
    for p in range(4):
        for which, line in enumerate((beside(a), above(a))):
            first_hop(p, a, line, which).start()
    for p in range(4):
        own_copy(p).start()
    r.small[a] = r.small_own[...]

    def iota(shape, dimension):
        return lax.broadcasted_iota(jnp.int32, shape, dimension)

    square = jnp.where(iota((KSEL, KSEL), 0) == iota((KSEL, KSEL), 1), 1.0, 0.0).astype(LOW)
    position = iota((KSEL, total), 1).astype(F32)
    for pair in range(lines * heads):
        line, head = pair // heads, pair % heads
        columns = dot_nt(square, r.chosen[pair].astype(F32).astype(LOW))
        for block in range(blocks):
            pick = head * blocks + block
            r.count_own[line, pick : pick + 1, :] = jnp.sum(
                jnp.where(columns[:, block : block + 1] == position, 1.0, 0.0),
                axis=0,
                keepdims=True,
            )
    for step in range(1, lines):
        count_copy(step - 1, (a + step) % lines, a).start()
    r.count[a] = r.count_own[a]

    NEAR, OVER, ACROSS = range(3)

    def gather(buffer, s, kind, j, owner, target, slot):
        view = buffer.at[s, j, row_block(owner - 1, owned)]
        return remote(
            view, view, r.ag_s.at[kind, j, slot], r.ag_r.at[kind, j, slot], tensor=target
        )

    def used_before(s, kind):
        return s > 0 if kind < 2 else s < lines - 1

    def gather_start(buffer, s, kind, j):
        @pl.when(used_before(s, kind))
        def _():
            gather_sent(buffer, s, kind, j)

        gather(buffer, s, kind, j, t, over_chip, OVER).start()
        gather(buffer, s, kind, j, t, across_chip, ACROSS).start()
        gather(buffer, s, kind, j, t, near_chip, NEAR).start()

    def gather_wait(buffer, s, kind, j):
        @pl.when(middle_chip)
        def _():
            gather(buffer, s, kind, j, across_chip, across_chip, ACROSS).wait_recv()

        @pl.when(end_chip)
        def _():
            gather(buffer, s, kind, j, near_chip, near_chip, NEAR).wait_recv()
            gather(buffer, s, kind, j, over_chip, over_chip, OVER).wait_recv()

    def gather_sent(buffer, s, kind, j):
        gather(buffer, s, kind, j, t, over_chip, OVER).wait_send()
        gather(buffer, s, kind, j, t, across_chip, ACROSS).wait_send()
        gather(buffer, s, kind, j, t, near_chip, NEAR).wait_send()

    def scatter(s, kind, j, owner, slot):
        return remote(
            r.part.at[kind, j, row_block(owner - 1, owned)],
            r.arrived.at[s, kind, j, slot],
            r.rs_s.at[kind, j, slot],
            r.rs_r.at[kind, j, slot],
            tensor=owner,
        )

    def scatter_start(s, kind, j, product):
        @pl.when(used_before(s, kind))
        def _():
            scatter_sent(s, kind, j)

        r.part[kind, j] = product.astype(LOW)

        @pl.when(end_chip)
        def _():
            scatter(s, kind, j, over_chip, OVER).start()
            scatter(s, kind, j, near_chip, NEAR).start()

        @pl.when(middle_chip)
        def _():
            scatter(s, kind, j, across_chip, ACROSS).start()

    def scatter_sum(s, kind, j):
        result = r.part[kind, j, mine].astype(F32)
        for slot in (NEAR, ACROSS, OVER):
            scatter(s, kind, j, t, slot).wait_recv()
            result = result + r.arrived[s, kind, j, slot].astype(F32)
        return result

    def scatter_sent(s, kind, j):
        @pl.when(end_chip)
        def _():
            scatter(s, kind, j, over_chip, OVER).wait_send()
            scatter(s, kind, j, near_chip, NEAR).wait_send()

        @pl.when(middle_chip)
        def _():
            scatter(s, kind, j, across_chip, ACROSS).wait_send()

    own_rows = (r.nrm, r.nmlp, r.ups, r.brn, r.act, r.gpre, r.mix, r.dqkv)
    all_rows = (
        r.all_nrm,
        r.all_nmlp,
        r.all_ups,
        r.all_brn,
        r.all_act,
        r.all_gpre,
        r.all_mix,
        r.all_dqkv,
    )

    def rows_copy(index, s, same, stays=False):
        core = c if same else 1 - c
        src = own_rows[index].at[s]
        dst = all_rows[index].at[a, c]
        if index <= BRN:
            src = src.at[:, :, row_block(core, half_width)]
        recv = r.heads_r.at[a] if index == DQKV else r.rows_r.at[index]
        if stays:
            return pltpu.make_async_copy(src, dst, recv)
        if same:
            return remote(src, dst, r.rows_s.at[index, s, 0], recv, section=s)
        return remote(src, dst, r.rows_s.at[index, s, 1], recv, section=s, seq=1 - c)

    passed_rows = {UPS: r.pass_ups, GPRE: r.pass_gpre}
    places = {UPS: 0, GPRE: 1}

    def detour_copy(index):
        return remote(
            own_rows[index].at[0],
            passed_rows[index],
            r.pass_s.at[places[index]],
            r.pass_r.at[places[index]],
            section=1,
        )

    def passed_copies(index):
        copies = []
        for step in range(2 if index <= BRN else 1):
            core = (c + step) % 2
            src = passed_rows[index]
            if index <= BRN:
                src = src.at[:, :, row_block(core, half_width)]
            send = r.pass_on_s.at[places[index], step]
            dst = all_rows[index].at[3, c]
            copies.append(remote(src, dst, send, r.rows_r.at[index], section=0, seq=core))
        return copies

    def pass_rows(index):
        @pl.when(a == 1)
        def _():
            detour_copy(index).wait_recv()
            for copy in passed_copies(index):
                copy.start()

    def goes_direct(index, s):
        return jnp.logical_not((a == 3) & (s == 0)) if index in passed_rows else a >= 0

    def rows_start(index, s):
        if index in passed_rows:

            @pl.when((a == 3) & (s == 0))
            def _():
                detour_copy(index).start()

        @pl.when(a == s)
        def _():
            rows_copy(index, s, True, True).start()

        @pl.when((a != s) & goes_direct(index, s))
        def _():
            rows_copy(index, s, True).start()

        if index <= BRN:

            @pl.when(goes_direct(index, s))
            def _():
                rows_copy(index, s, False).start()

    def forward_rows(s):
        for index in (NRM, MIX, NMLP, ACT):
            rows_start(index, s)

    def rows_sent(index, s):
        @pl.when((a != s) & goes_direct(index, s))
        def _():
            rows_copy(index, s, True).wait_send()

        if index <= BRN:

            @pl.when(goes_direct(index, s))
            def _():
                rows_copy(index, s, False).wait_send()

    def share_copy(index, core):
        view = all_rows[index].at[:, core]
        return remote(view, view, r.share_s.at[index - ACT], r.share_r.at[index - ACT], seq=1 - c)

    def share_heads(line, core):
        view = r.all_dqkv.at[line, core]
        return remote(view, view, r.heads_s.at[line], r.heads_sr.at[line], seq=1 - c)

    def share(index):
        drain(all_rows[index].at[:, c], r.rows_r.at[index])
        share_copy(index, c).start()

    def norm_copy(s):
        return remote(
            r.norm_part.at[s], r.norm_all.at[a], r.norm_s.at[s], r.norm_r, section=s
        )

    def norm_start(s):
        @pl.when(a == s)
        def _():
            pltpu.make_async_copy(r.norm_part.at[s], r.norm_all.at[a], r.norm_r).start()

        @pl.when(a != s)
        def _():
            norm_copy(s).start()

    def home_copy(what, s, j):
        src, dst, send, recv = what
        chip = 2 * j + t - 1
        return remote(src.at[s, j], dst.at[a], send.at[s, j], recv, section=s, tensor=chip)

    def home_start(what, s):
        @pl.when(middle_chip)
        def _():
            for j in streams:
                home_copy(what, s, j).start()

    def home_sent(what, s):
        @pl.when(middle_chip)
        def _():
            for j in streams:
                home_copy(what, s, j).wait_send()

    out_home = (r.out_low, r.acts, r.out_s, r.out_r)
    grad_home = (r.grad_low, r.grads, r.grad_s, r.grad_r)

    length = r.lengths[a // buckets, a % buckets]
    key = iota((stream_rows, total), 1)
    for j in streams:
        query = c * local + j * stream_rows + iota((stream_rows, total), 0)
        r.near[j] = jnp.where((query >= key) & (query - key < WIN), 1.0, 0.0)
    key_row = iota((1, total), 1)

    def row_mask(place):
        return jnp.where(place < length, 1.0, 0.0)

    def stream_mask(j):
        return row_mask(c * local + j * stream_rows + iota((stream_rows, 1), 0))

    def multiplicity(s, j, head):
        block = j * stream_rows // QB
        pick = head * blocks + block
        limit = (c * blocks + block) * QB - WIN
        return r.near[j] + jnp.where(key_row <= limit, r.count[s, pick : pick + 1, :], 0.0)

    def head_cols(head):
        return slice(head * HDIM, (head + 1) * HDIM)

    def kv_copy(s, j):
        view = r.kv.at[s, :, j * stream_rows : (j + 1) * stream_rows]
        return remote(view, view, r.kv_s.at[s, j], r.kv_r.at[s, j], seq=1 - c)

    def dkv_copy(s):
        return remote(r.dkv_out.at[s], r.dkv_in.at[s], r.dkv_s.at[s], r.dkv_r.at[s], seq=1 - c)

    def own_sequence(ref):
        both = ref[a // buckets].astype(F32)
        picked = both[:, 0, :]
        for bucket in range(1, buckets):
            picked = jnp.where(a % buckets == bucket, both[:, bucket, :], picked)
        return picked

    def first_copy(stream):
        return remote(
            r.first_out, r.first_in.at[stream], r.first_s, r.first_r.at[stream], tensor=1 + t % 2
        )

    own_place = c * local + t * rows + iota((rows, 1), 0)
    r.first_out[0] = own_sequence(r.inputs).astype(LOW)
    r.first_out[1] = (own_sequence(r.cotangent) * row_mask(own_place)).astype(LOW)
    first_copy(t // 2).start()
    r.norm_part[...] = jnp.zeros_like(r.norm_part)

    def first_rows(j):
        @pl.when(middle_chip)
        def _():
            first_copy(j).wait_recv()
            r.hidden[j] = r.first_in[j, 0].astype(F32)
            r.upstream[j] = r.first_in[j, 1]

    def on_owner(stage):
        def run(s, j):
            @pl.when(middle_chip)
            def _():
                stage(s, j)

        return run

    @on_owner
    def enter(s, j):
        xhat, inverse = standard(r.hidden[j])
        r.xhat1[s, j] = xhat
        r.inv1[s, j] = jnp.broadcast_to(inverse, (owned, 128))
        r.nrm[s, j, mine] = (xhat * r.small[s, 0:1] + r.small[s, 1:2]).astype(LOW)
        gather_start(r.nrm, s, 0, j)

    def project(s, j):
        gather_wait(r.nrm, s, 0, j)
        normed = r.nrm[s, j]
        place = row_block(c * STREAMS + j, stream_rows)
        bias_v = r.small[s, 7:8, half_width : half_width + head_width]
        key_rows = dot_nt(normed, r.wq[s, head_width : 2 * head_width])
        value_rows = dot_nt(normed, r.wq[s, 2 * head_width : 3 * head_width]) + bias_v
        r.kv[s, 0, place] = key_rows.astype(LOW)
        r.kv[s, 1, place] = value_rows.astype(LOW)

    def ask(s, j):
        queries = dot_nt(r.nrm[s, j], r.wq[s, 0:head_width]) + r.small[s, 7:8, :head_width]
        r.qry[s, j] = queries.astype(LOW)

    def attend_line(s, j):
        mixed = []
        for head in range(heads):
            cols = head_cols(head)
            times = multiplicity(s, j, head)
            scores = scale * dot_nt(r.qry[s, j, :, cols], r.kv[s, 0, :, cols])
            scores = jnp.where(times > 0.0, scores, MASKED)
            top = jnp.max(scores, axis=-1, keepdims=True)
            terms = times * jnp.exp(scores - top)
            weights = terms / jnp.sum(terms, axis=-1, keepdims=True)
            r.soft[s, j, head] = weights
            mixed.append(dot_nn(weights.astype(LOW), r.kv[s, 1, :, cols]))
        r.mix[s, j] = (jnp.concatenate(mixed, axis=-1) * stream_mask(j)).astype(LOW)

    def leave_attention(s, j):
        scatter_start(s, 0, j, dot_nn(r.mix[s, j], r.wo[s]))

    @on_owner
    def between(s, j):
        middle = r.hidden[j] + scatter_sum(s, 0, j) + r.small[s, 4:5]
        r.middle[j] = middle
        xhat, inverse = standard(middle)
        r.xhat2[s, j] = xhat
        r.inv2[s, j] = jnp.broadcast_to(inverse, (owned, 128))
        r.nmlp[s, j, mine] = (xhat * r.small[s, 2:3] + r.small[s, 3:4]).astype(LOW)
        gather_start(r.nmlp, s, 1, j)

    def feed(s, j):
        gather_wait(r.nmlp, s, 1, j)
        before = dot_nn(r.nmlp[s, j], r.wf[s]) + r.small[s, 6:7, :units]
        bend = jnp.tanh(0.7978845608028654 * (before + 0.044715 * before * before * before))
        r.act[s, j] = (0.5 * before * (1.0 + bend)).astype(LOW)
        r.slope[s, j] = 0.5 * (1.0 + bend) + 0.5 * before * (1.0 - bend * bend) * (
            0.7978845608028654 * (1.0 + 3 * 0.044715 * before * before)
        )


    def leave_feed(s, j):
        scatter_start(s, 1, j, dot_nn(r.act[s, j], r.wp[s]))

    @on_owner
    def finish(s, j):
        result = r.middle[j] + scatter_sum(s, 1, j) + r.small[s, 5:6]
        r.out_low[s, j] = result.astype(LOW)
        r.hidden[j] = result.astype(LOW).astype(F32)

    def small_ready(s):
        @pl.when(a != s)
        def _():
            small_copy(0, a, s).wait_recv()

    small_ready(0)
    for j in streams:
        first_rows(j)
        enter(0, j)

    def forward(s, _):
        need(s, 0)
        need(s, 1)

        @pl.when(a != s)
        def _():
            count_copy(0, a, s).wait_recv()

        for j in streams:
            project(s, j)

            @pl.when(c == 0)
            def _():
                kv_copy(s, j).start()

            ask(s, j)
            if j == 0:

                @pl.when(c == 1)
                def _():
                    for other in streams:
                        kv_copy(s, other).wait_recv()

            attend_line(s, j)
            leave_attention(s, j)

        @pl.when(s == 0)
        def _():
            pass_all(0, (2,))
            for later in range(1, lines):
                pass_all(later, (0, 1, 2))

        @pl.when(s == 1)
        def _():
            pass_far(1, 2)
            pass_far(1, 3)
            for later in range(2, lines):
                for p in range(4):
                    pass_far(later, p)

        for j in streams:
            between(s, j)
        @pl.when(s == 0)
        def _():
            for later in range(lines):
                pass_all(later, (3,))

        need(s, 2)
        for j in streams:
            feed(s, j)
            if j == 0:
                need(s, 3)
            leave_feed(s, j)


        @pl.when(s >= 2)
        def _():
            forward_rows(s - 2)


        @pl.when(s + 1 < lines)
        def _():
            small_ready(s + 1)

        for j in streams:
            finish(s, j)

            @pl.when(s + 1 < lines)
            def _():
                enter(s + 1, j)

        home_start(out_home, s)

        @pl.when(s == 0)
        def _():
            pass_far(1, 0)
            pass_far(1, 1)

        return 0

    lax.fori_loop(0, lines, forward, 0)

    @on_owner
    def turn(s, j):
        upstream = r.upstream[j]
        r.ups[s, j, mine] = upstream
        gather_start(r.ups, s, 2, j)
        r.norm_part[s, 5:6] += column_sum(upstream)

    def feed_back(s, j):
        gather_wait(r.ups, s, 2, j)
        grad_pre = (dot_nt(r.ups[s, j], r.wp[s]) * r.slope[s, j]).astype(LOW)
        r.gpre[s, j] = grad_pre
        scatter_start(s, 2, j, dot_nt(grad_pre, r.wf[s]))
        r.norm_part[s, 6:7, :units] += column_sum(grad_pre)

    @on_owner
    def between_back(s, j):
        grad = scatter_sum(s, 2, j)
        xhat = r.xhat2[s, j]
        upstream = r.upstream[j].astype(F32)
        grad_middle = upstream + standard_back(
            grad * r.small[s, 2:3], xhat, r.inv2[s, j, :, 0:1]
        )
        r.middle[j] = grad_middle
        branch = grad_middle.astype(LOW)
        r.brn[s, j, mine] = branch
        gather_start(r.brn, s, 3, j)
        r.norm_part[s, 2:3] += column_sum(grad * xhat)
        r.norm_part[s, 3:4] += column_sum(grad)
        r.norm_part[s, 4:5] += column_sum(branch)

    def mixed_back(s, j):
        gather_wait(r.brn, s, 3, j)
        r.gmix[j] = (dot_nt(r.brn[s, j], r.wo[s]) * stream_mask(j)).astype(LOW)

    def attend_line_back(s, j):
        grad_q, grad_k, grad_v = [], [], []
        for head in range(heads):
            cols = head_cols(head)
            weights = r.soft[s, j, head]
            grad_head = r.gmix[j, :, cols]
            grad_weights = dot_nt(grad_head, r.kv[s, 1, :, cols])
            inner = jnp.sum(weights * grad_weights, axis=-1, keepdims=True)
            grad_scores = (weights * (grad_weights - inner)).astype(LOW)
            grad_k.append(scale * dot_tn(grad_scores, r.qry[s, j, :, cols]))
            grad_v.append(dot_tn(weights.astype(LOW), grad_head))
            grad_q.append(scale * dot_nn(grad_scores, r.kv[s, 0, :, cols]))
        for which, grad in enumerate((grad_k, grad_v)):
            grad = jnp.concatenate(grad, axis=-1)
            r.dkv_all[which] = grad if j == STREAMS - 1 else r.dkv_all[which] + grad
        grad_q = jnp.concatenate(grad_q, axis=-1).astype(LOW)
        r.dqkv[s, 0, j] = grad_q
        r.norm_part[s, 7:8, :head_width] += column_sum(grad_q)

    def join_keys(s, j):
        for which in range(2):
            joined = r.dkv_all[which, row_block(c * STREAMS + j, stream_rows)].astype(LOW)
            r.dqkv[s, 1 + which, j] = joined
            if which == 1:
                lanes = slice(half_width, half_width + head_width)
                r.norm_part[s, 7:8, lanes] += column_sum(joined)

    def leave_back(s, j):
        product = dot_nn(r.dqkv[s, 0, j], r.wq[s, 0:head_width])
        for which in range(1, 3):
            weight = r.wq[s, which * head_width : (which + 1) * head_width]
            product = product + dot_nn(r.dqkv[s, which, j], weight)
        scatter_start(s, 3, j, product)

    @on_owner
    def finish_back(s, j):
        grad = scatter_sum(s, 3, j)
        xhat = r.xhat1[s, j]
        result = r.middle[j] + standard_back(
            grad * r.small[s, 0:1], xhat, r.inv1[s, j, :, 0:1]
        )
        r.upstream[j] = result.astype(LOW)
        r.grad_low[s, j] = result.astype(LOW)
        r.norm_part[s, 0:1] += column_sum(grad * xhat)
        r.norm_part[s, 1:2] += column_sum(grad)

    last_first = tuple(reversed(streams))
    for j in last_first:
        turn(lines - 1, j)

    def backward(index, _):
        s = lines - 1 - index
        for j in last_first:
            feed_back(s, j)
        rows_start(UPS, s)
        rows_start(GPRE, s)

        @pl.when(index < 2)
        def _():
            forward_rows(lines - 2 + index)

        @pl.when(index == lines - 1)
        def _():
            share(ACT)
            share(MIX)

        for j in last_first:
            between_back(s, j)
        for j in last_first:
            mixed_back(s, j)
            if j == 0:
                rows_start(BRN, s)
            attend_line_back(s, j)

            @pl.when(c == 1)
            def _():
                join_keys(s, j)
                leave_back(s, j)

        @pl.when(c == 1)
        def _():
            r.dkv_out[s] = r.dkv_all[:, 0:local].astype(LOW)
            dkv_copy(s).start()

        @pl.when(c == 0)
        def _():
            dkv_copy(s).wait_recv()
            r.dkv_all[:, 0:local] += r.dkv_in[s].astype(F32)
            for j in last_first:
                join_keys(s, j)
                leave_back(s, j)

        rows_start(DQKV, s)

        @pl.when(s == 0)
        def _():
            pass_rows(UPS)
            pass_rows(GPRE)

        for j in last_first:
            finish_back(s, j)

            @pl.when(s > 0)
            def _():
                turn(s - 1, j)

        norm_start(s)
        home_start(grad_home, s)
        return 0

    lax.fori_loop(0, lines, backward, 0)

    loads = [
        pltpu.make_async_copy(source, target, r.load_sem.at[place])
        for place, (source, target) in enumerate(
            (
                (r.all_nmlp, r.row_nmlp),
                (r.all_ups, r.row_ups),
                (r.all_act, r.row_act),
                (r.all_gpre, r.row_gpre),
            )
        )
    ]
    stores = [
        pltpu.make_async_copy(r.own_proj, r.grad_proj, r.store_sem.at[0]),
        pltpu.make_async_copy(r.own_fc, r.grad_fc, r.store_sem.at[1]),
    ]
    share(GPRE)
    drain(r.all_nmlp, r.rows_r.at[NMLP])
    loads[0].start()
    share_copy(ACT, 1 - c).wait_recv()
    loads[2].start()
    drain(r.all_ups, r.rows_r.at[UPS])
    loads[1].start()
    share_copy(GPRE, 1 - c).wait_recv()
    loads[3].start()

    def every_row(ref):
        return ref[...].reshape(lines * total, ref.shape[-1])

    loads[1].wait()
    loads[2].wait()
    r.own_proj[...] = dot_tn(every_row(r.row_act), every_row(r.row_ups))
    stores[0].start()
    loads[0].wait()
    loads[3].wait()
    r.own_fc[...] = dot_tn(every_row(r.row_nmlp), every_row(r.row_gpre))
    stores[1].start()
    for line in range(lines):
        drain(r.all_dqkv.at[line, c], r.heads_r.at[line])
        share_heads(line, c).start()

    drain(r.norm_all, r.norm_r)
    slot = c * chips + t
    norm_sum = r.norm_all[0]
    for line in range(1, lines):
        norm_sum = norm_sum + r.norm_all[line]
    r.ends[slot] = norm_sum

    def ends_copy(step):
        core, chip = step // chips, step % chips
        view = r.ends.at[slot]
        return remote(
            view,
            view,
            r.ends_s.at[step - 1],
            r.ends_r,
            seq=(c + core) % 2,
            tensor=(t + chip) % chips,
        )

    for step in range(1, 2 * chips):
        ends_copy(step).start()

    for index in (UPS, GPRE):

        @pl.when(a == 3)
        def _():
            detour_copy(index).wait_send()

        @pl.when(a == 1)
        def _():
            for copy in passed_copies(index):
                copy.wait_send()

    for kind, buffer in enumerate((r.nrm, r.nmlp, r.ups, r.brn)):
        for j in streams:
            scatter_sent(0, kind, j)

            @pl.when(middle_chip)
            def _():
                gather_sent(buffer, 0, kind, j)

    for index in (NRM, BRN):
        drain(all_rows[index], r.rows_r.at[index])
    for written in stores:
        written.wait()
    share_copy(MIX, 1 - c).wait_recv()
    for index in range(ACT, DQKV):
        share_copy(index, c).wait_send()
    for line in range(lines):
        share_heads(line, 1 - c).wait_recv()
        share_heads(line, c).wait_send()
    drain(r.acts, r.out_r)
    drain(r.grads, r.grad_r)
    drain(r.ends.at[0 : 2 * chips - 1], r.ends_r)
    for step in range(1, 2 * chips):
        ends_copy(step).wait_send()
    for step in range(1, lines):
        small_copy(step - 1, (a + step) % lines, a).wait_send()
        count_copy(step - 1, (a + step) % lines, a).wait_send()
    for p in range(4):
        for which, line in enumerate((beside(a), above(a))):
            first_hop(p, a, line, which).wait_send()

    first_copy(t // 2).wait_send()

    def sent(s, _):
        home_sent(out_home, s)
        home_sent(grad_home, s)

        @pl.when(a != s)
        def _():
            norm_copy(s).wait_send()

        @pl.when(c == 0)
        def _():
            for j in streams:
                kv_copy(s, j).wait_send()

        @pl.when(c == 1)
        def _():
            dkv_copy(s).wait_send()

        for index in range(8):
            rows_sent(index, s)
        for p in range(4):

            @pl.when((a == beside(s)) | (a == above(s)))
            def _():
                second_hop(p, s, 0).wait_send()

            @pl.when(a != s)
            def _():
                core_hop(p, s, c).wait_send()

        return 0

    lax.fori_loop(0, lines, sent, 0)


def relay_call(inputs, cotangent, lengths, chosen, singles, weights):
    lines = lax.axis_size("section")
    chips = lax.axis_size("tensor")
    rows, buckets, width = inputs.shape[1:]
    local, total, half = rows * chips, 2 * rows * chips, width // 2
    head_width, units = weights["wo_in"].shape[0], weights["wp_in"].shape[0]
    heads = head_width // HDIM
    stream = local // STREAMS
    peers, owned = chips - 1, stream // 2
    vmem, dma = pltpu.VMEM, pltpu.SemaphoreType.DMA
    operands = dict(
        inputs=inputs,
        cotangent=cotangent,
        lengths=lengths,
        chosen=chosen,
        **singles,
        **weights,
    )

    def space(name):
        if name in weights:
            return pl.ANY
        return pltpu.SMEM if operands[name] is lengths else pltpu.VMEM

    sums = dict(
        acts=((lines, rows, width), LOW),
        grads=((lines, rows, width), LOW),
        ends=((2 * chips, 8, width), F32),
    )
    gathered = dict(
        all_nrm=((lines, 2, STREAMS, stream, half), LOW),
        all_nmlp=((lines, 2, STREAMS, stream, half), LOW),
        all_ups=((lines, 2, STREAMS, stream, half), LOW),
        all_brn=((lines, 2, STREAMS, stream, half), LOW),
        all_act=((lines, 2, STREAMS, stream, units), LOW),
        all_gpre=((lines, 2, STREAMS, stream, units), LOW),
        all_mix=((lines, 2, STREAMS, stream, head_width), LOW),
        all_dqkv=((lines, 2, 3, STREAMS, stream, head_width), LOW),
    )
    products = dict(grad_proj=((units, half), F32), grad_fc=((half, units), F32))
    outputs = dict(**sums, **gathered, **products)
    scratch = dict(
        wq=vmem((lines,) + weights["wq_in"].shape, LOW),
        wo=vmem((lines,) + weights["wo_in"].shape, LOW),
        wf=vmem((lines,) + weights["wf_in"].shape, LOW),
        wp=vmem((lines,) + weights["wp_in"].shape, LOW),
        small_own=vmem((8, width), F32),
        small=vmem((lines, 8, width), F32),
        count_own=vmem((lines, 8, total), F32),
        count=vmem((lines, 8, total), F32),
        hidden=vmem((STREAMS, owned, width), F32),
        middle=vmem((STREAMS, owned, width), F32),
        upstream=vmem((STREAMS, owned, width), LOW),
        first_out=vmem((2, owned, width), LOW),
        first_in=vmem((STREAMS, 2, owned, width), LOW),
        xhat1=vmem((lines, STREAMS, owned, width), F32),
        inv1=vmem((lines, STREAMS, owned, 128), F32),
        xhat2=vmem((lines, STREAMS, owned, width), F32),
        inv2=vmem((lines, STREAMS, owned, 128), F32),
        nrm=vmem((lines, STREAMS, stream, width), LOW),
        nmlp=vmem((lines, STREAMS, stream, width), LOW),
        ups=vmem((lines, STREAMS, stream, width), LOW),
        brn=vmem((lines, STREAMS, stream, width), LOW),
        act=vmem((lines, STREAMS, stream, units), LOW),
        gpre=vmem((lines, STREAMS, stream, units), LOW),
        slope=vmem((lines, STREAMS, stream, units), F32),
        mix=vmem((lines, STREAMS, stream, head_width), LOW),
        qry=vmem((lines, STREAMS, stream, head_width), LOW),
        gmix=vmem((STREAMS, stream, head_width), LOW),
        dqkv=vmem((lines, 3, STREAMS, stream, head_width), LOW),
        row_nmlp=vmem(gathered["all_nmlp"][0], LOW),
        row_ups=vmem(gathered["all_ups"][0], LOW),
        row_act=vmem(gathered["all_act"][0], LOW),
        row_gpre=vmem(gathered["all_gpre"][0], LOW),
        own_proj=vmem((units, half), F32),
        own_fc=vmem((half, units), F32),
        pass_ups=vmem((STREAMS, stream, width), LOW),
        pass_gpre=vmem((STREAMS, stream, units), LOW),
        kv=vmem((lines, 2, total, head_width), LOW),
        soft=vmem((lines, STREAMS, heads, stream, total), F32),
        near=vmem((STREAMS, stream, total), F32),
        dkv_all=vmem((2, total, head_width), F32),
        dkv_out=vmem((lines, 2, local, head_width), LOW),
        dkv_in=vmem((lines, 2, local, head_width), LOW),
        part=vmem((4, STREAMS, stream, width), LOW),
        arrived=vmem((lines, 4, STREAMS, peers, owned, width), LOW),
        out_low=vmem((lines, STREAMS, owned, width), LOW),
        grad_low=vmem((lines, STREAMS, owned, width), LOW),
        norm_part=vmem((lines, 8, width), F32),
        norm_all=vmem((lines, 8, width), F32),
        w_first_s=dma((4, 2)),
        w_first_r=dma((lines, 4)),
        w_second_s=dma((lines, 4)),
        w_second_r=dma((lines, 4, 2)),
        w_core_s=dma((lines, 4)),
        w_core_r=dma((lines, 4)),
        w_own=dma((4,)),
        small_s=dma((lines - 1,)),
        small_r=dma((lines,)),
        count_s=dma((lines - 1,)),
        count_r=dma((lines,)),
        ag_s=dma((4, STREAMS, peers)),
        ag_r=dma((4, STREAMS, peers)),
        rs_s=dma((4, STREAMS, peers)),
        rs_r=dma((4, STREAMS, peers)),
        kv_s=dma((lines, STREAMS)),
        kv_r=dma((lines, STREAMS)),
        dkv_s=dma((lines,)),
        dkv_r=dma((lines,)),
        rows_s=dma((8, lines, 2)),
        rows_r=dma((8,)),
        load_sem=dma((4,)),
        store_sem=dma((2,)),
        pass_s=dma((2,)),
        pass_r=dma((2,)),
        pass_on_s=dma((2, 2)),
        share_s=dma((4,)),
        share_r=dma((4,)),
        heads_r=dma((lines,)),
        heads_s=dma((lines,)),
        heads_sr=dma((lines,)),
        first_s=dma,
        first_r=dma((STREAMS,)),
        out_s=dma((lines, STREAMS)),
        out_r=dma,
        grad_s=dma((lines, STREAMS)),
        grad_r=dma,
        norm_s=dma((lines,)),
        norm_r=dma,
        ends_s=dma((2 * chips - 1,)),
        ends_r=dma,
    )
    names = tuple(operands) + tuple(outputs) + tuple(scratch)
    results = pl.pallas_call(
        functools.partial(relay_kernel, names),
        out_shape=[jax.ShapeDtypeStruct(shape, kind) for shape, kind in outputs.values()],
        in_specs=[pl.BlockSpec(memory_space=space(name)) for name in operands],
        out_specs=[
            pl.BlockSpec(memory_space=pltpu.VMEM if name in sums else pl.ANY)
            for name in outputs
        ],
        scratch_shapes=list(scratch.values()),
        compiler_params=pltpu.CompilerParams(
            collective_id=0, has_side_effects=True, vmem_limit_bytes=60 * 2**20
        ),
        name="relay",
    )(*operands.values())
    return dict(zip(outputs, results))


def weights_kernel(names, *refs):
    r = types.SimpleNamespace(**dict(zip(names, refs)))
    micro_count, rows, buckets, width = r.activations.shape
    chips, units, head_width = r.ends.shape[0] // 2, r.grad_proj.shape[0], r.all_mix.shape[-1]
    lines = r.acts.shape[0]
    loads = [
        pltpu.make_async_copy(source, target, r.load_sem.at[place])
        for place, (source, target) in enumerate(
            (
                (r.all_mix, r.mix),
                (r.all_brn, r.brn),
                (r.all_nrm, r.nrm),
                (r.all_dqkv, r.dqkv),
            )
        )
    ]
    stores = [
        pltpu.make_async_copy(source, target, r.store_sem.at[place])
        for place, (source, target) in enumerate(
            (
                (r.grad_proj, r.w_proj),
                (r.grad_fc, r.w_fc),
                (r.own_out, r.w_out),
                (r.own_qkv, r.w_qkv),
            )
        )
    ]
    for load in loads:
        load.start()
    stores[0].start()
    stores[1].start()

    sums = r.ends[0]
    for other in range(1, 2 * chips):
        sums = sums + r.ends[other]
    singles = (r.ln1_gain, r.ln1_shift, r.ln2_gain, r.ln2_shift, r.b_out, r.b_proj)
    for place, single in enumerate(singles):
        single[...] = sums[place : place + 1]
    for chip in range(chips):
        both = r.ends[chip] + r.ends[chips + chip]
        r.b_fc[:, chip * units : (chip + 1) * units] = both[6:7, :units]
        here = slice(chip * head_width, (chip + 1) * head_width)
        r.b_qv[0:1, here] = both[7:8, :head_width]
        r.b_qv[1:2, here] = both[7:8, width // 2 : width // 2 + head_width]
    for target, source in ((r.activations, r.acts), (r.in_grads, r.grads)):
        for micro in range(micro_count):
            rows_of = [
                source[micro * buckets + bucket].astype(F32)[:, None, :]
                for bucket in range(buckets)
            ]
            target[micro] = jnp.concatenate(rows_of, axis=1).astype(LOW)

    def flat(array):
        return array.reshape(lines * 2 * chips * rows, array.shape[-1])

    loads[0].wait()
    loads[1].wait()
    r.own_out[...] = dot_tn(flat(r.mix[...]), flat(r.brn[...]))
    stores[2].start()
    loads[2].wait()
    loads[3].wait()
    nrm = flat(r.nrm[...])
    for which in range(3):
        r.own_qkv[which] = dot_tn(flat(r.dqkv[:, :, which]), nrm)
    stores[3].start()
    for store in stores:
        store.wait()


def weights_call(relayed, inputs_shape, head_width, units):
    chips = lax.axis_size("tensor")
    width = inputs_shape[-1]
    half = width // 2
    outputs = dict(
        activations=(inputs_shape, LOW),
        in_grads=(inputs_shape, LOW),
        ln1_gain=((1, width), F32),
        ln1_shift=((1, width), F32),
        w_qkv=((3, head_width, half), F32),
        b_qv=((2, width), F32),
        w_out=((head_width, half), F32),
        b_out=((1, width), F32),
        ln2_gain=((1, width), F32),
        ln2_shift=((1, width), F32),
        w_fc=((half, units), F32),
        b_fc=((1, chips * units), F32),
        w_proj=((units, half), F32),
        b_proj=((1, width), F32),
    )
    rows = ("mix", "brn", "nrm", "dqkv")
    own = dict(own_out="w_out", own_qkv="w_qkv")
    copied = ("w_proj", "w_fc", "w_out", "w_qkv")
    scratch = {name: pltpu.VMEM(relayed["all_" + name].shape, LOW) for name in rows}
    scratch.update({name: pltpu.VMEM(outputs[of][0], F32) for name, of in own.items()})
    scratch["load_sem"] = pltpu.SemaphoreType.DMA((4,))
    scratch["store_sem"] = pltpu.SemaphoreType.DMA((4,))
    whole, apart = pl.BlockSpec(memory_space=pltpu.VMEM), pl.BlockSpec(memory_space=pl.ANY)
    small = ("acts", "grads", "ends")
    return pl.pallas_call(
        functools.partial(weights_kernel, tuple(relayed) + tuple(outputs) + tuple(scratch)),
        out_shape=[jax.ShapeDtypeStruct(shape, kind) for shape, kind in outputs.values()],
        in_specs=[whole if name in small else apart for name in relayed],
        out_specs=[apart if name in copied else whole for name in outputs],
        scratch_shapes=list(scratch.values()),
        compiler_params=pltpu.CompilerParams(vmem_limit_bytes=60 * 2**20),
        name="weight_gradients",
    )(*relayed.values())


def on_line(
    inputs,
    cotangent,
    lengths,
    chosen,
    ln1_gain,
    ln1_shift,
    w_qkv,
    b_qv,
    w_out,
    b_out,
    ln2_gain,
    ln2_shift,
    w_fc,
    b_fc,
    w_proj,
    b_proj,
):
    head_width, units = w_out.shape[1], w_fc.shape[2]
    singles = dict(
        ln1_gain=ln1_gain,
        ln1_shift=ln1_shift,
        ln2_gain=ln2_gain,
        ln2_shift=ln2_shift,
        b_out=b_out,
        b_proj=b_proj,
        b_fc=b_fc,
        b_qv=b_qv[0],
    )
    weights = dict(
        wq_in=jnp.swapaxes(w_qkv[0], 1, 2).reshape(-1, inputs.shape[-1]),
        wo_in=w_out[0],
        wf_in=w_fc[0],
        wp_in=w_proj[0],
    )
    picks = chosen.reshape((-1,) + chosen.shape[-2:])
    relayed = relay_call(inputs, cotangent, lengths, picks, singles, weights)
    results = list(weights_call(relayed, inputs.shape, head_width, units))
    results[4] = jnp.swapaxes(results[4], 1, 2)
    vectors = (2, 3, 7, 8, 9, 11, 13)
    return tuple(
        result if place in vectors else result[None] for place, result in enumerate(results)
    )


def fits_lines(mesh):
    return mesh.shape["section"] == 4 and mesh.shape["seq"] == 2 and mesh.shape["tensor"] == 4


def solution(mesh):
    placed = (
        P(None, ("seq", "tensor"), None, None),
        P(None, ("seq", "tensor"), None, None),
        P(),
        P("section", None, None, "tensor", "seq", None),
        P("section", None),
        P("section", None),
        P("section", None, None, "tensor"),
        P("section", None, "tensor"),
        P("section", "tensor", None),
        P("section", None),
        P("section", None),
        P("section", None),
        P("section", None, "tensor"),
        P("section", "tensor"),
        P("section", "tensor", None),
        P("section", None),
    )
    return jax.shard_map(
        on_line if fits_lines(mesh) else on_device,
        mesh=mesh,
        in_specs=placed,
        out_specs=(
            P("section", None, ("seq", "tensor"), None, None),
            P("section", None, ("seq", "tensor"), None, None),
            P("section", None),
            P("section", None),
            P("section", None, "seq", "tensor"),
            P("section", None, None),
            P("section", "tensor", "seq"),
            P("section", None),
            P("section", None),
            P("section", None),
            P("section", "seq", "tensor"),
            P("section", None),
            P("section", "tensor", "seq"),
            P("section", None),
        ),
        check_vma=False,
    )
```

```python
import functools
import types

import jax
import jax.numpy as jnp
from jax import lax
from jax.experimental import pallas as pl
from jax.experimental.pallas import tpu as pltpu
from jax.sharding import PartitionSpec as P

HDIM = 64
WIN = 64
QB = 64
KSEL = 64


NORM_EPS = 1e-05
MASKED = -1000000000.0


def from_behind(value, axis, steps):
    count = lax.axis_size(axis)
    first, last = (max(0, -steps), min(count, count - steps))
    return lax.ppermute(value, axis, [(source, source + steps) for source in range(first, last)])


def layer_norm(values, gain, shift):
    average = jnp.mean(values, axis=-1, keepdims=True)
    centred = values - average
    variance = jnp.mean(centred * centred, axis=-1, keepdims=True)
    return centred * lax.rsqrt(variance + NORM_EPS) * gain + shift


def gelu_tanh(values):
    return (
        0.5
        * values
        * (1.0 + jnp.tanh(0.7978845608028654 * (values + 0.044715 * values * values * values)))
    )


def gather_rows(row_block):
    return lax.all_gather(row_block, "tensor", axis=0, tiled=True)


def scatter_product(left_rows, weight, formula):
    return lax.psum_scatter(
        jnp.einsum(formula, left_rows, weight, preferred_element_type=jnp.float32).astype(
            jnp.bfloat16
        ),
        "tensor",
        scatter_dimension=0,
        tiled=True,
    ).astype(jnp.float32)


def near_slabs(full_rows, seq_start, seq_first, length_local):
    buckets = full_rows.shape[1]
    heads_local = full_rows.shape[2] // HDIM
    blocks = length_local // QB
    earlier = lax.dynamic_slice_in_dim(full_rows, jnp.maximum(seq_start - WIN, 0), WIN, 0)
    earlier = jnp.where(seq_first, jnp.zeros_like(earlier), earlier)
    local_part = lax.dynamic_slice_in_dim(full_rows, seq_start, length_local, 0)
    segment = jnp.concatenate([earlier, local_part], 0).reshape(
        length_local + WIN, buckets, heads_local, HDIM
    )
    return jnp.concatenate(
        [
            segment[offset_index * QB : offset_index * QB + length_local].reshape(
                blocks, QB, buckets, heads_local, HDIM
            )
            for offset_index in range(WIN // QB + 1)
        ],
        1,
    )


def far_rows(full_rows, flat_index):
    total_rows, buckets, feature_width = full_rows.shape
    heads_local = feature_width // HDIM
    return jnp.take(full_rows.reshape(total_rows * buckets * heads_local, HDIM), flat_index, axis=0)


def key_geometry(chosen_now, seq_start, blocks):
    buckets, heads_local = (chosen_now.shape[0], chosen_now.shape[1])
    bucket_ids = lax.broadcasted_iota(jnp.int32, chosen_now.shape, 0)
    head_ids = lax.broadcasted_iota(jnp.int32, chosen_now.shape, 1)
    flat_index = (chosen_now * buckets + bucket_ids) * heads_local + head_ids
    block_start = seq_start + QB * lax.broadcasted_iota(jnp.int32, (blocks, 1, 1), 0)
    query_ids = lax.broadcasted_iota(jnp.int32, (1, QB, 1), 1)
    key_ids = lax.broadcasted_iota(jnp.int32, (1, 1, WIN + QB), 2)
    distance = query_ids + WIN - key_ids
    near_ok = (distance >= 0) & (distance < WIN) & (block_start + key_ids - WIN >= 0)
    far_ok = chosen_now + WIN <= block_start.reshape(1, 1, blocks, 1)
    near_mask = jnp.broadcast_to(
        near_ok[:, None, None], (blocks, buckets, heads_local, QB, WIN + QB)
    )
    far_mask = jnp.broadcast_to(
        jnp.transpose(far_ok, (2, 0, 1, 3))[:, :, :, None, :],
        (blocks, buckets, heads_local, QB, KSEL),
    )
    return (flat_index, jnp.concatenate([near_mask, far_mask], -1))


def attention_setup(queries, key_rows, value_rows, chosen_now, seq_start, seq_first):
    length_local, buckets, feature_width = queries.shape
    heads_local = feature_width // HDIM
    blocks = length_local // QB
    query_blocks = queries.reshape(blocks, QB, buckets, heads_local, HDIM)
    flat_index, key_mask = key_geometry(chosen_now, seq_start, blocks)
    near_keys = near_slabs(key_rows, seq_start, seq_first, length_local)
    near_values = near_slabs(value_rows, seq_start, seq_first, length_local)
    far_keys = far_rows(key_rows, flat_index)
    far_values = far_rows(value_rows, flat_index)
    near_scores = jnp.einsum(
        "bqnhe,btnhe->bnhqt", query_blocks, near_keys, preferred_element_type=jnp.float32
    )
    far_scores = jnp.einsum(
        "bqnhe,nhbke->bnhqk", query_blocks, far_keys, preferred_element_type=jnp.float32
    )
    scores = jnp.where(
        key_mask, HDIM ** (-0.5) * jnp.concatenate([near_scores, far_scores], -1), MASKED
    )
    return (query_blocks, near_keys, near_values, far_keys, far_values, flat_index, scores)


def attend(queries, key_rows, value_rows, chosen_now, seq_start, seq_first):
    query_blocks, near_keys, near_values, far_keys, far_values, flat_index, scores = (
        attention_setup(queries, key_rows, value_rows, chosen_now, seq_start, seq_first)
    )
    span = WIN + QB
    row_top = jnp.max(scores, -1, keepdims=True)
    exp_terms = jnp.exp(scores - row_top)
    row_total = jnp.sum(exp_terms, -1, keepdims=True)
    softmax_low = (exp_terms / row_total).astype(jnp.bfloat16)
    near_part = jnp.einsum(
        "bnhqt,btnhe->bqnhe",
        softmax_low[..., :span],
        near_values,
        preferred_element_type=jnp.float32,
    )
    far_part = jnp.einsum(
        "bnhqk,nhbke->bqnhe",
        softmax_low[..., span:],
        far_values,
        preferred_element_type=jnp.float32,
    )
    return ((near_part + far_part).reshape(queries.shape), row_top + jnp.log(row_total))


def spread_back(near_grad, far_grad, flat_index, seq_start, seq_first, total_rows):
    blocks, span, buckets, heads_local, head_size = near_grad.shape
    length_local = blocks * QB
    feature_width = heads_local * head_size
    segment = jnp.zeros((length_local + WIN, buckets, heads_local, head_size), jnp.float32)
    for offset_index in range(WIN // QB + 1):
        piece = near_grad[:, offset_index * QB : (offset_index + 1) * QB].reshape(
            length_local, buckets, heads_local, head_size
        )
        segment = segment.at[offset_index * QB : offset_index * QB + length_local].add(piece)
    full_rows = jnp.zeros((total_rows * buckets * heads_local, head_size), jnp.float32)
    full_rows = full_rows.at[flat_index.reshape(-1)].add(far_grad.reshape(-1, head_size))
    full_rows = full_rows.reshape(total_rows, buckets, feature_width)
    local_part = segment[WIN:].reshape(length_local, buckets, feature_width)
    earlier = jnp.where(seq_first, 0.0, segment[:WIN].reshape(WIN, buckets, feature_width))
    full_rows = lax.dynamic_update_slice_in_dim(
        full_rows,
        lax.dynamic_slice_in_dim(full_rows, seq_start, length_local, 0) + local_part,
        seq_start,
        0,
    )
    earlier_start = jnp.maximum(seq_start - WIN, 0)
    full_rows = lax.dynamic_update_slice_in_dim(
        full_rows,
        lax.dynamic_slice_in_dim(full_rows, earlier_start, WIN, 0) + earlier,
        earlier_start,
        0,
    )
    return full_rows


def attend_back(
    queries, key_rows, value_rows, chosen_now, seq_start, seq_first, log_total, grad_mixed
):
    query_blocks, near_keys, near_values, far_keys, far_values, flat_index, scores = (
        attention_setup(queries, key_rows, value_rows, chosen_now, seq_start, seq_first)
    )
    span = WIN + QB
    score_scale = HDIM ** (-0.5)
    grad_blocks = grad_mixed.reshape(query_blocks.shape)
    weights_full = jnp.exp(scores - log_total)
    softmax_low = weights_full.astype(jnp.bfloat16)
    grad_near_weights = jnp.einsum(
        "bqnhe,btnhe->bnhqt", grad_blocks, near_values, preferred_element_type=jnp.float32
    )
    grad_far_weights = jnp.einsum(
        "bqnhe,nhbke->bnhqk", grad_blocks, far_values, preferred_element_type=jnp.float32
    )
    grad_weights = jnp.concatenate([grad_near_weights, grad_far_weights], -1)
    row_dot = jnp.sum(weights_full * grad_weights, -1, keepdims=True)
    grad_scores = (weights_full * (grad_weights - row_dot)).astype(jnp.bfloat16)
    grad_near, grad_far = (grad_scores[..., :span], grad_scores[..., span:])
    grad_queries = score_scale * (
        jnp.einsum("bnhqt,btnhe->bqnhe", grad_near, near_keys, preferred_element_type=jnp.float32)
        + jnp.einsum("bnhqk,nhbke->bqnhe", grad_far, far_keys, preferred_element_type=jnp.float32)
    )
    near_key_grad = score_scale * jnp.einsum(
        "bnhqt,bqnhe->btnhe", grad_near, query_blocks, preferred_element_type=jnp.float32
    )
    far_key_grad = score_scale * jnp.einsum(
        "bnhqk,bqnhe->nhbke", grad_far, query_blocks, preferred_element_type=jnp.float32
    )
    near_value_grad = jnp.einsum(
        "bnhqt,bqnhe->btnhe",
        softmax_low[..., :span],
        grad_blocks,
        preferred_element_type=jnp.float32,
    )
    far_value_grad = jnp.einsum(
        "bnhqk,bqnhe->nhbke",
        softmax_low[..., span:],
        grad_blocks,
        preferred_element_type=jnp.float32,
    )
    total_rows = key_rows.shape[0]
    key_grad = spread_back(
        near_key_grad, far_key_grad, flat_index, seq_start, seq_first, total_rows
    )
    value_grad = spread_back(
        near_value_grad, far_value_grad, flat_index, seq_start, seq_first, total_rows
    )
    return (grad_queries.reshape(queries.shape), key_grad, value_grad)


def forward_pass(hidden, params, chosen_now, query_mask, seq_start, seq_first, finish):
    (
        ln1_gain,
        ln1_shift,
        w_qkv,
        b_qv,
        w_out,
        b_out,
        ln2_gain,
        ln2_shift,
        w_fc,
        b_fc,
        w_proj,
        b_proj,
    ) = params
    hidden_wide = hidden.astype(jnp.float32)
    normed_all = gather_rows(layer_norm(hidden_wide, ln1_gain, ln1_shift).astype(jnp.bfloat16))
    projected = jnp.einsum("pnd,jdc->jpnc", normed_all, w_qkv, preferred_element_type=jnp.float32)
    queries = (projected[0] + b_qv[0]).astype(jnp.bfloat16)
    key_rows, value_rows = (
        lax.all_gather(projected[1].astype(jnp.bfloat16), "seq", axis=0, tiled=True),
        lax.all_gather((projected[2] + b_qv[1]).astype(jnp.bfloat16), "seq", axis=0, tiled=True),
    )
    attended, log_total = attend(queries, key_rows, value_rows, chosen_now, seq_start, seq_first)
    mixed_rows = (attended * query_mask[:, :, None]).astype(jnp.bfloat16)
    middle = hidden_wide + scatter_product(mixed_rows, w_out, "pnc,cd->pnd") + b_out
    normed_mlp = gather_rows(layer_norm(middle, ln2_gain, ln2_shift).astype(jnp.bfloat16))
    pre_active = (
        jnp.einsum("pnd,df->pnf", normed_mlp, w_fc, preferred_element_type=jnp.float32) + b_fc
    )
    active = gelu_tanh(pre_active).astype(jnp.bfloat16)
    if not finish:
        return (
            normed_all,
            queries,
            key_rows,
            value_rows,
            log_total,
            mixed_rows,
            middle,
            normed_mlp,
            pre_active,
            active,
        )
    output = (middle + scatter_product(active, w_proj, "pnf,fd->pnd") + b_proj).astype(jnp.bfloat16)
    return (output, (key_rows, value_rows))


def backward_pass(hidden, upstream, params, chosen_now, query_mask, seq_start, seq_first):
    (
        ln1_gain,
        ln1_shift,
        w_qkv,
        b_qv,
        w_out,
        b_out,
        ln2_gain,
        ln2_shift,
        w_fc,
        b_fc,
        w_proj,
        b_proj,
    ) = params
    (
        normed_all,
        queries,
        key_rows,
        value_rows,
        log_total,
        mixed_rows,
        middle,
        normed_mlp,
        pre_active,
        active,
    ) = forward_pass(hidden, params, chosen_now, query_mask, seq_start, seq_first, False)
    upstream_all = gather_rows(upstream)
    grad_w_proj = jnp.einsum(
        "pnf,pnd->fd", active, upstream_all, preferred_element_type=jnp.float32
    )
    grad_b_proj = jnp.sum(upstream.astype(jnp.float32), axis=(0, 1))
    grad_active = jnp.einsum(
        "pnd,fd->pnf", upstream_all, w_proj, preferred_element_type=jnp.float32
    )
    unused_value, gelu_pull = jax.vjp(gelu_tanh, pre_active)
    grad_pre = gelu_pull(grad_active)[0].astype(jnp.bfloat16)
    grad_w_fc = jnp.einsum("pnd,pnf->df", normed_mlp, grad_pre, preferred_element_type=jnp.float32)
    grad_b_fc = jnp.sum(grad_pre.astype(jnp.float32), axis=(0, 1))
    grad_normed_mlp = scatter_product(grad_pre, w_fc, "pnf,df->pnd")
    unused_norm, second_pull = jax.vjp(layer_norm, middle, ln2_gain, ln2_shift)
    grad_mid_norm, grad_ln2_gain, grad_ln2_shift = second_pull(grad_normed_mlp)
    grad_middle = upstream.astype(jnp.float32) + grad_mid_norm
    grad_branch = grad_middle.astype(jnp.bfloat16)
    grad_b_out = jnp.sum(grad_branch.astype(jnp.float32), axis=(0, 1))
    branch_all = gather_rows(grad_branch)
    grad_w_out = jnp.einsum(
        "pnc,pnd->cd", mixed_rows, branch_all, preferred_element_type=jnp.float32
    )
    grad_mixed = jnp.einsum(
        "pnd,cd->pnc", branch_all, w_out, preferred_element_type=jnp.float32
    ).astype(jnp.bfloat16) * query_mask[:, :, None].astype(jnp.bfloat16)
    grad_queries, key_grad_all, value_grad_all = attend_back(
        queries, key_rows, value_rows, chosen_now, seq_start, seq_first, log_total, grad_mixed
    )
    key_grad, value_grad = (
        lax.psum_scatter(
            key_grad_all.astype(jnp.bfloat16), "seq", scatter_dimension=0, tiled=True
        ).astype(jnp.float32),
        lax.psum_scatter(
            value_grad_all.astype(jnp.bfloat16), "seq", scatter_dimension=0, tiled=True
        ).astype(jnp.float32),
    )
    grad_project = jnp.stack(
        [
            grad_queries.astype(jnp.bfloat16),
            key_grad.astype(jnp.bfloat16),
            value_grad.astype(jnp.bfloat16),
        ],
        2,
    )
    grad_w_qkv = jnp.einsum(
        "pnd,pnjc->jdc", normed_all, grad_project, preferred_element_type=jnp.float32
    )
    grad_b_qv = jnp.sum(grad_project[:, :, 0::2].astype(jnp.float32), axis=(0, 1))
    grad_normed = scatter_product(grad_project, w_qkv, "pnjc,jdc->pnd")
    unused_first, first_pull = jax.vjp(layer_norm, hidden.astype(jnp.float32), ln1_gain, ln1_shift)
    grad_in_norm, grad_ln1_gain, grad_ln1_shift = first_pull(grad_normed)
    grad_hidden = (grad_middle + grad_in_norm).astype(jnp.bfloat16)
    block_grads = (
        grad_ln1_gain,
        grad_ln1_shift,
        grad_w_qkv,
        grad_b_qv,
        grad_w_out,
        grad_b_out,
        grad_ln2_gain,
        grad_ln2_shift,
        grad_w_fc,
        grad_b_fc,
        grad_w_proj,
        grad_b_proj,
    )
    return (grad_hidden, block_grads)


def on_device(
    inputs,
    cotangent,
    lengths,
    chosen,
    ln1_gain,
    ln1_shift,
    w_qkv,
    b_qv,
    w_out,
    b_out,
    ln2_gain,
    ln2_shift,
    w_fc,
    b_fc,
    w_proj,
    b_proj,
):
    params = tuple(
        (
            weight_array[0]
            for weight_array in (
                ln1_gain,
                ln1_shift,
                w_qkv,
                b_qv,
                w_out,
                b_out,
                ln2_gain,
                ln2_shift,
                w_fc,
                b_fc,
                w_proj,
                b_proj,
            )
        )
    )
    section_index = lax.axis_index("section")
    section_count = lax.axis_size("section")
    seq_index = lax.axis_index("seq")
    tensor_index = lax.axis_index("tensor")
    tensor_count = lax.axis_size("tensor")
    micro_count, rows_local, buckets, feature_width = inputs.shape
    length_local = rows_local * tensor_count
    heads_width = w_qkv.shape[-1]
    seq_start = seq_index * length_local
    seq_first = seq_index == 0
    positions = seq_start + lax.broadcasted_iota(jnp.int32, (micro_count, length_local, buckets), 1)
    mask_all = (positions < lengths[:, None, :]).astype(jnp.float32)
    mask_rows = lax.dynamic_slice_in_dim(mask_all, tensor_index * rows_local, rows_local, 1)
    step_count = micro_count + section_count - 1
    chosen_section = chosen[0]
    received = jnp.zeros((rows_local, buckets, feature_width), jnp.bfloat16)
    stored = jnp.zeros((micro_count, rows_local, buckets, feature_width), jnp.bfloat16)
    outputs = jnp.zeros_like(stored)
    for step_index in range(step_count):
        micro_index = step_index - section_index
        running = (micro_index >= 0) & (micro_index < micro_count)
        slot_index = jnp.clip(micro_index, 0, micro_count - 1)
        block_in = jnp.where(
            section_index == 0, lax.dynamic_index_in_dim(inputs, slot_index, 0, False), received
        )
        chosen_now = lax.dynamic_index_in_dim(chosen_section, slot_index, 0, False)
        query_mask = lax.dynamic_index_in_dim(mask_all, slot_index, 0, False)
        result, key_pair = forward_pass(
            block_in, params, chosen_now, query_mask, seq_start, seq_first, True
        )
        stored = jnp.where(
            running, lax.dynamic_update_index_in_dim(stored, block_in, slot_index, 0), stored
        )
        outputs = jnp.where(
            running, lax.dynamic_update_index_in_dim(outputs, result, slot_index, 0), outputs
        )
        received = from_behind(result, "section", 1)
    back_received = jnp.zeros((rows_local, buckets, feature_width), jnp.bfloat16)
    in_grads = jnp.zeros_like(stored)
    totals = None
    for step_index in range(step_count):
        micro_index = step_index - (section_count - 1 - section_index)
        running = (micro_index >= 0) & (micro_index < micro_count)
        slot_index = jnp.clip(micro_index, 0, micro_count - 1)
        chosen_now = lax.dynamic_index_in_dim(chosen_section, slot_index, 0, False)
        query_mask = lax.dynamic_index_in_dim(mask_all, slot_index, 0, False)
        local_mask = lax.dynamic_index_in_dim(mask_rows, slot_index, 0, False)
        top_grad = (
            lax.dynamic_index_in_dim(cotangent, slot_index, 0, False).astype(jnp.float32)
            * local_mask[:, :, None]
        ).astype(jnp.bfloat16)
        upstream = jnp.where(section_index == section_count - 1, top_grad, back_received)
        hidden = lax.dynamic_index_in_dim(stored, slot_index, 0, False)
        grad_hidden, block_grads = backward_pass(
            hidden, upstream, params, chosen_now, query_mask, seq_start, seq_first
        )
        block_grads = tuple(
            (jnp.where(running, grad_part, jnp.zeros_like(grad_part)) for grad_part in block_grads)
        )
        totals = (
            block_grads
            if step_index == 0
            else tuple(
                (total_part + grad_part for total_part, grad_part in zip(totals, block_grads))
            )
        )
        in_grads = jnp.where(
            running, lax.dynamic_update_index_in_dim(in_grads, grad_hidden, slot_index, 0), in_grads
        )
        back_received = from_behind(grad_hidden, "section", -1)
    (
        sum_ln1_gain,
        sum_ln1_shift,
        sum_w_qkv,
        sum_b_qv,
        sum_w_out,
        sum_b_out,
        sum_ln2_gain,
        sum_ln2_shift,
        sum_w_fc,
        sum_b_fc,
        sum_w_proj,
        sum_b_proj,
    ) = totals
    part_qkv, part_out, part_fc, part_proj = (
        lax.psum_scatter(
            sum_w_qkv.astype(jnp.bfloat16), "seq", scatter_dimension=1, tiled=True
        ).astype(jnp.float32),
        lax.psum_scatter(
            sum_w_out.astype(jnp.bfloat16), "seq", scatter_dimension=1, tiled=True
        ).astype(jnp.float32),
        lax.psum_scatter(
            sum_w_fc.astype(jnp.bfloat16), "seq", scatter_dimension=0, tiled=True
        ).astype(jnp.float32),
        lax.psum_scatter(
            sum_w_proj.astype(jnp.bfloat16), "seq", scatter_dimension=1, tiled=True
        ).astype(jnp.float32),
    )
    bias_qv = lax.dynamic_update_slice_in_dim(
        jnp.zeros((2, feature_width), jnp.float32), sum_b_qv, tensor_index * heads_width, 1
    )
    units_local = sum_b_fc.shape[0]
    bias_fc = lax.dynamic_update_slice_in_dim(
        jnp.zeros((units_local * tensor_count,), jnp.float32),
        sum_b_fc,
        tensor_index * units_local,
        0,
    )
    small_sums = lax.psum(
        (
            sum_ln1_gain,
            sum_ln1_shift,
            bias_qv,
            sum_b_out,
            sum_ln2_gain,
            sum_ln2_shift,
            bias_fc,
            sum_b_proj,
        ),
        ("seq", "tensor"),
    )
    return (
        outputs[None],
        in_grads[None],
        small_sums[0][None],
        small_sums[1][None],
        part_qkv[None],
        small_sums[2][None],
        part_out[None],
        small_sums[3][None],
        small_sums[4][None],
        small_sums[5][None],
        part_fc[None],
        small_sums[6][None],
        part_proj[None],
        small_sums[7][None],
    )


STREAMS = 2
NRM, NMLP, UPS, BRN, ACT, GPRE, MIX, DQKV = range(8)
F32 = jnp.float32
LOW = jnp.bfloat16
MESH_ID = pl.DeviceIdType.MESH


def dot_nn(left, right):
    return lax.dot_general(left, right, (((1,), (0,)), ((), ())), preferred_element_type=F32)


def dot_nt(left, right):
    return lax.dot_general(left, right, (((1,), (1,)), ((), ())), preferred_element_type=F32)


def dot_tn(left, right):
    return lax.dot_general(left, right, (((0,), (0,)), ((), ())), preferred_element_type=F32)


def standard(rows):
    centred = rows - jnp.mean(rows, axis=-1, keepdims=True)
    scale = lax.rsqrt(jnp.mean(centred * centred, axis=-1, keepdims=True) + NORM_EPS)
    return centred * scale, scale


def standard_back(grad, xhat, scale):
    inner = jnp.mean(grad * xhat, axis=-1, keepdims=True)
    return scale * (grad - jnp.mean(grad, axis=-1, keepdims=True) - xhat * inner)


def column_sum(rows):
    return jnp.sum(rows.astype(F32), axis=0, keepdims=True)


def relay_kernel(names, *refs):
    r = types.SimpleNamespace(**dict(zip(names, refs)))
    a, c, t = (lax.axis_index(name) for name in ("section", "seq", "tensor"))
    lines = lax.axis_size("section")
    chips = lax.axis_size("tensor")
    rows, buckets, width = r.inputs.shape[1:]
    half_width = width // 2
    local = rows * chips
    total = 2 * local
    stream_rows = local // STREAMS
    head_width = r.wo_in.shape[0]
    heads = head_width // HDIM
    blocks = local // QB
    units = r.wp_in.shape[0]
    scale = HDIM ** (-0.5)
    streams = range(STREAMS)

    def remote(src, dst, send, recv, **target):
        return pltpu.make_async_remote_copy(
            src_ref=src,
            dst_ref=dst,
            send_sem=send,
            recv_sem=recv,
            device_id=target,
            device_id_type=MESH_ID,
        )

    def drain(ref, sem):
        pltpu.make_async_copy(ref, ref, sem).wait()

    def row_block(index, size):
        return pl.ds(pl.multiple_of(index * size, size), size)

    near_chip = t + 1 - 2 * (t % 2)
    over_chip = (t + 2) % 4
    across_chip = 3 - t
    middle_chip = (t == 1) | (t == 2)
    end_chip = (t == 0) | (t == 3)
    owned = stream_rows // 2
    mine = row_block(t - 1, owned)
    my_half = row_block(c, local)

    def store(p):
        return (r.wq, r.wo, r.wf, r.wp)[p]

    def source(p):
        return (r.wq_in, r.wo_in, r.wf_in, r.wp_in)[p]

    def own_copy(p):
        return pltpu.make_async_copy(source(p), store(p).at[a], r.w_own.at[p])

    for p in range(4):
        own_copy(p).start()

    r.kv[...] = jnp.zeros(r.kv.shape, LOW)

    barrier = pltpu.get_barrier_semaphore()
    greeted = 0
    for line in range(lines):
        for chip in range(chips):
            for core in range(2):
                if (line, chip, core) != (0, 0, 0) and (core == 0 or line * chip == 0):
                    there = {
                        "section": (a + line) % lines,
                        "seq": (c + core) % 2,
                        "tensor": (t + chip) % chips,
                    }
                    pl.semaphore_signal(barrier, inc=1, device_id=there, device_id_type=MESH_ID)
                    greeted += 1
    pl.semaphore_wait(barrier, greeted)

    def beside(s):
        return s + 1 - 2 * (s % 2)

    def above(s):
        return (s + 2) % 4

    def height(p):
        return source(p).shape[0]

    def core_half(p, s, core):
        return store(p).at[s, row_block(core, height(p) // 2)]

    def first_hop(p, s, neighbour, which):
        return remote(
            core_half(p, s, c),
            core_half(p, s, c),
            r.w_first_s.at[p, which],
            r.w_first_r.at[s, p],
            section=neighbour,
        )

    def second_hop(p, s, which):
        view = store(p).at[s, row_block(2 * c + which, height(p) // 4)]
        return remote(
            view, view, r.w_second_s.at[s, p], r.w_second_r.at[s, p, which], section=3 - s
        )

    def core_hop(p, s, core):
        view = core_half(p, s, core)
        return remote(view, view, r.w_core_s.at[s, p], r.w_core_r.at[s, p], seq=1 - c)

    def pass_on(s, p, which):
        line = (beside(s), above(s))[which]

        @pl.when(a == line)
        def _():
            first_hop(p, s, line, which).wait_recv()
            second_hop(p, s, which).start()
            core_hop(p, s, c).start()

    def pass_all(s, pieces):
        for p in pieces:
            for which in range(2):
                pass_on(s, p, which)

    def pass_far(s, p):
        @pl.when(a == 3 - s)
        def _():
            second_hop(p, s, 0).wait_recv()
            second_hop(p, s, 1).wait_recv()
            core_hop(p, s, c).start()

    def need(s, p):
        @pl.when(s == 0)
        def _():
            if p < 2:
                pass_all(0, (p,))
            pass_far(0, p)

        @pl.when(a != s)
        def _():
            core_hop(p, s, 1 - c).wait_recv()

    def small_copy(step, line, slot):
        return remote(
            r.small_own, r.small.at[slot], r.small_s.at[step], r.small_r.at[slot], section=line
        )

    def count_copy(step, line, slot):
        return remote(
            r.count_own.at[line],
            r.count.at[slot],
            r.count_s.at[step],
            r.count_r.at[slot],
            section=line,
        )

    singles = (r.ln1_gain, r.ln1_shift, r.ln2_gain, r.ln2_shift, r.b_out, r.b_proj)
    for place, single in enumerate(singles):
        r.small_own[place : place + 1] = single[...]
    r.small_own[6:7, :units] = r.b_fc[...]
    r.small_own[7:8, :head_width] = r.b_qv[0:1]
    r.small_own[7:8, half_width : half_width + head_width] = r.b_qv[1:2]
    for step in range(1, lines):
        small_copy(step - 1, (a + step) % lines, a).start()
    for p in range(4):
        own_copy(p).wait()
        for which, line in enumerate((beside(a), above(a))):
            first_hop(p, a, line, which).start()
    r.small[a] = r.small_own[...]

    def iota(shape, dimension):
        return lax.broadcasted_iota(jnp.int32, shape, dimension)

    square = jnp.where(iota((KSEL, KSEL), 0) == iota((KSEL, KSEL), 1), 1.0, 0.0).astype(LOW)
    position = iota((KSEL, total), 1).astype(F32)
    for pair in range(lines * heads):
        line, head = pair // heads, pair % heads
        columns = dot_nt(square, r.chosen[pair].astype(F32).astype(LOW))
        for block in range(blocks):
            pick = head * blocks + block
            r.count_own[line, pick : pick + 1, :] = jnp.sum(
                jnp.where(columns[:, block : block + 1] == position, 1.0, 0.0),
                axis=0,
                keepdims=True,
            )
    for step in range(1, lines):
        count_copy(step - 1, (a + step) % lines, a).start()
    r.count[a] = r.count_own[a]

    NEAR, OVER, ACROSS = range(3)

    def gather(buffer, s, kind, j, owner, target, slot):
        view = buffer.at[s, j, row_block(owner - 1, owned)]
        return remote(
            view, view, r.ag_s.at[kind, j, slot], r.ag_r.at[kind, j, slot], tensor=target
        )

    def used_before(s, kind):
        return s > 0 if kind < 2 else s < lines - 1

    def gather_start(buffer, s, kind, j):
        @pl.when(used_before(s, kind))
        def _():
            gather_sent(buffer, s, kind, j)

        gather(buffer, s, kind, j, t, over_chip, OVER).start()
        gather(buffer, s, kind, j, t, across_chip, ACROSS).start()
        gather(buffer, s, kind, j, t, near_chip, NEAR).start()

    def gather_wait(buffer, s, kind, j):
        @pl.when(middle_chip)
        def _():
            gather(buffer, s, kind, j, across_chip, across_chip, ACROSS).wait_recv()

        @pl.when(end_chip)
        def _():
            gather(buffer, s, kind, j, near_chip, near_chip, NEAR).wait_recv()
            gather(buffer, s, kind, j, over_chip, over_chip, OVER).wait_recv()

    def gather_sent(buffer, s, kind, j):
        gather(buffer, s, kind, j, t, over_chip, OVER).wait_send()
        gather(buffer, s, kind, j, t, across_chip, ACROSS).wait_send()
        gather(buffer, s, kind, j, t, near_chip, NEAR).wait_send()

    def scatter(s, kind, j, owner, slot):
        return remote(
            r.part.at[kind, j, row_block(owner - 1, owned)],
            r.arrived.at[s, kind, j, slot],
            r.rs_s.at[kind, j, slot],
            r.rs_r.at[kind, j, slot],
            tensor=owner,
        )

    def scatter_start(s, kind, j, product):
        @pl.when(used_before(s, kind))
        def _():
            scatter_sent(s, kind, j)

        r.part[kind, j] = product.astype(LOW)

        @pl.when(end_chip)
        def _():
            scatter(s, kind, j, over_chip, OVER).start()
            scatter(s, kind, j, near_chip, NEAR).start()

        @pl.when(middle_chip)
        def _():
            scatter(s, kind, j, across_chip, ACROSS).start()

    def scatter_sum(s, kind, j):
        result = r.part[kind, j, mine].astype(F32)
        for slot in (NEAR, ACROSS, OVER):
            scatter(s, kind, j, t, slot).wait_recv()
            result = result + r.arrived[s, kind, j, slot].astype(F32)
        return result

    def scatter_sent(s, kind, j):
        @pl.when(end_chip)
        def _():
            scatter(s, kind, j, over_chip, OVER).wait_send()
            scatter(s, kind, j, near_chip, NEAR).wait_send()

        @pl.when(middle_chip)
        def _():
            scatter(s, kind, j, across_chip, ACROSS).wait_send()

    own_rows = (r.nrm, r.nmlp, r.ups, r.brn, r.act, r.gpre, r.mix, r.dqkv)
    all_rows = (
        r.all_nrm,
        r.all_nmlp,
        r.all_ups,
        r.all_brn,
        r.all_act,
        r.all_gpre,
        r.all_mix,
        r.all_dqkv,
    )

    def rows_copy(index, s, same, stays=False):
        core = c if same else 1 - c
        src = own_rows[index].at[s]
        dst = all_rows[index].at[a, c]
        if index <= BRN:
            src = src.at[:, :, row_block(core, half_width)]
        recv = r.heads_r.at[a] if index == DQKV else r.rows_r.at[index]
        if stays:
            return pltpu.make_async_copy(src, dst, recv)
        if same:
            return remote(src, dst, r.rows_s.at[index, s, 0], recv, section=s)
        return remote(src, dst, r.rows_s.at[index, s, 1], recv, section=s, seq=1 - c)

    passed_rows = {UPS: r.pass_ups, GPRE: r.pass_gpre}
    places = {UPS: 0, GPRE: 1}

    def detour_copy(index):
        return remote(
            own_rows[index].at[0],
            passed_rows[index],
            r.pass_s.at[places[index]],
            r.pass_r.at[places[index]],
            section=1,
        )

    def passed_copies(index):
        copies = []
        for step in range(2 if index <= BRN else 1):
            core = (c + step) % 2
            src = passed_rows[index]
            if index <= BRN:
                src = src.at[:, :, row_block(core, half_width)]
            send = r.pass_on_s.at[places[index], step]
            dst = all_rows[index].at[3, c]
            copies.append(remote(src, dst, send, r.rows_r.at[index], section=0, seq=core))
        return copies

    def pass_rows(index):
        @pl.when(a == 1)
        def _():
            detour_copy(index).wait_recv()
            for copy in passed_copies(index):
                copy.start()

    def goes_direct(index, s):
        return jnp.logical_not((a == 3) & (s == 0)) if index in passed_rows else a >= 0

    def rows_start(index, s):
        if index in passed_rows:

            @pl.when((a == 3) & (s == 0))
            def _():
                detour_copy(index).start()

        @pl.when(a == s)
        def _():
            rows_copy(index, s, True, True).start()

        @pl.when((a != s) & goes_direct(index, s))
        def _():
            rows_copy(index, s, True).start()

        if index <= BRN:

            @pl.when(goes_direct(index, s))
            def _():
                rows_copy(index, s, False).start()

    def forward_rows(s):
        for index in (NRM, MIX, NMLP, ACT):
            rows_start(index, s)

    def rows_sent(index, s):
        @pl.when((a != s) & goes_direct(index, s))
        def _():
            rows_copy(index, s, True).wait_send()

        if index <= BRN:

            @pl.when(goes_direct(index, s))
            def _():
                rows_copy(index, s, False).wait_send()

    def share_copy(index, core):
        view = all_rows[index].at[:, core]
        return remote(view, view, r.share_s.at[index - ACT], r.share_r.at[index - ACT], seq=1 - c)

    def share_heads(line, core):
        view = r.all_dqkv.at[line, core]
        return remote(view, view, r.heads_s.at[line], r.heads_sr.at[line], seq=1 - c)

    def share(index):
        drain(all_rows[index].at[:, c], r.rows_r.at[index])
        share_copy(index, c).start()

    def norm_copy(s):
        return remote(
            r.norm_part.at[s], r.norm_all.at[a], r.norm_s.at[s], r.norm_r, section=s
        )

    def norm_start(s):
        @pl.when(a == s)
        def _():
            pltpu.make_async_copy(r.norm_part.at[s], r.norm_all.at[a], r.norm_r).start()

        @pl.when(a != s)
        def _():
            norm_copy(s).start()

    def home_copy(what, s, j):
        src, dst, send, recv = what
        chip = 2 * j + t - 1
        return remote(src.at[s, j], dst.at[a], send.at[s, j], recv, section=s, tensor=chip)

    def home_start(what, s):
        @pl.when(middle_chip)
        def _():
            for j in streams:
                home_copy(what, s, j).start()

    def home_sent(what, s):
        @pl.when(middle_chip)
        def _():
            for j in streams:
                home_copy(what, s, j).wait_send()

    out_home = (r.out_low, r.acts, r.out_s, r.out_r)
    grad_home = (r.grad_low, r.grads, r.grad_s, r.grad_r)

    length = r.lengths[a // buckets, a % buckets]
    key = iota((stream_rows, total), 1)
    for j in streams:
        query = c * local + j * stream_rows + iota((stream_rows, total), 0)
        r.near[j] = jnp.where((query >= key) & (query - key < WIN), 1.0, 0.0)
    key_row = iota((1, total), 1)

    def row_mask(place):
        return jnp.where(place < length, 1.0, 0.0)

    def stream_mask(j):
        return row_mask(c * local + j * stream_rows + iota((stream_rows, 1), 0))

    def multiplicity(s, j, head):
        block = j * stream_rows // QB
        pick = head * blocks + block
        limit = (c * blocks + block) * QB - WIN
        return r.near[j] + jnp.where(key_row <= limit, r.count[s, pick : pick + 1, :], 0.0)

    def head_cols(head):
        return slice(head * HDIM, (head + 1) * HDIM)

    def kv_copy(s, j):
        view = r.kv.at[s, :, j * stream_rows : (j + 1) * stream_rows]
        return remote(view, view, r.kv_s.at[s, j], r.kv_r.at[s, j], seq=1 - c)

    def dkv_copy(s):
        return remote(r.dkv_out.at[s], r.dkv_in.at[s], r.dkv_s.at[s], r.dkv_r.at[s], seq=1 - c)

    def own_sequence(ref):
        both = ref[a // buckets].astype(F32)
        picked = both[:, 0, :]
        for bucket in range(1, buckets):
            picked = jnp.where(a % buckets == bucket, both[:, bucket, :], picked)
        return picked

    def first_copy(stream):
        return remote(
            r.first_out, r.first_in.at[stream], r.first_s, r.first_r.at[stream], tensor=1 + t % 2
        )

    own_place = c * local + t * rows + iota((rows, 1), 0)
    r.first_out[0] = own_sequence(r.inputs).astype(LOW)
    r.first_out[1] = (own_sequence(r.cotangent) * row_mask(own_place)).astype(LOW)
    first_copy(t // 2).start()
    r.norm_part[...] = jnp.zeros_like(r.norm_part)

    def first_rows(j):
        @pl.when(middle_chip)
        def _():
            first_copy(j).wait_recv()
            r.hidden[j] = r.first_in[j, 0].astype(F32)
            r.upstream[j] = r.first_in[j, 1]

    def on_owner(stage):
        def run(s, j):
            @pl.when(middle_chip)
            def _():
                stage(s, j)

        return run

    @on_owner
    def enter(s, j):
        xhat, inverse = standard(r.hidden[j])
        r.xhat1[s, j] = xhat
        r.inv1[s, j] = jnp.broadcast_to(inverse, (owned, 128))
        r.nrm[s, j, mine] = (xhat * r.small[s, 0:1] + r.small[s, 1:2]).astype(LOW)
        gather_start(r.nrm, s, 0, j)

    def project(s, j):
        gather_wait(r.nrm, s, 0, j)
        normed = r.nrm[s, j]
        place = row_block(c * STREAMS + j, stream_rows)
        bias_v = r.small[s, 7:8, half_width : half_width + head_width]
        key_rows = dot_nt(normed, r.wq[s, head_width : 2 * head_width])
        value_rows = dot_nt(normed, r.wq[s, 2 * head_width : 3 * head_width]) + bias_v
        r.kv[s, 0, place] = key_rows.astype(LOW)
        r.kv[s, 1, place] = value_rows.astype(LOW)

    def ask(s, j):
        queries = dot_nt(r.nrm[s, j], r.wq[s, 0:head_width]) + r.small[s, 7:8, :head_width]
        r.qry[s, j] = queries.astype(LOW)

    def attend_line(s, j):
        mixed = []
        for head in range(heads):
            cols = head_cols(head)
            times = multiplicity(s, j, head)
            scores = scale * dot_nt(r.qry[s, j, :, cols], r.kv[s, 0, :, cols])
            scores = jnp.where(times > 0.0, scores, MASKED)
            top = jnp.max(scores, axis=-1, keepdims=True)
            terms = times * jnp.exp(scores - top)
            weights = terms / jnp.sum(terms, axis=-1, keepdims=True)
            r.soft[s, j, head] = weights
            mixed.append(dot_nn(weights.astype(LOW), r.kv[s, 1, :, cols]))
        r.mix[s, j] = (jnp.concatenate(mixed, axis=-1) * stream_mask(j)).astype(LOW)

    def leave_attention(s, j):
        scatter_start(s, 0, j, dot_nn(r.mix[s, j], r.wo[s]))

    @on_owner
    def between(s, j):
        middle = r.hidden[j] + scatter_sum(s, 0, j) + r.small[s, 4:5]
        r.middle[j] = middle
        xhat, inverse = standard(middle)
        r.xhat2[s, j] = xhat
        r.inv2[s, j] = jnp.broadcast_to(inverse, (owned, 128))
        r.nmlp[s, j, mine] = (xhat * r.small[s, 2:3] + r.small[s, 3:4]).astype(LOW)
        gather_start(r.nmlp, s, 1, j)

    def feed(s, j):
        gather_wait(r.nmlp, s, 1, j)
        before = dot_nn(r.nmlp[s, j], r.wf[s]) + r.small[s, 6:7, :units]
        bend = jnp.tanh(0.7978845608028654 * (before + 0.044715 * before * before * before))
        r.act[s, j] = (0.5 * before * (1.0 + bend)).astype(LOW)
        r.slope[s, j] = 0.5 * (1.0 + bend) + 0.5 * before * (1.0 - bend * bend) * (
            0.7978845608028654 * (1.0 + 3 * 0.044715 * before * before)
        )


    def leave_feed(s, j):
        scatter_start(s, 1, j, dot_nn(r.act[s, j], r.wp[s]))

    @on_owner
    def finish(s, j):
        result = r.middle[j] + scatter_sum(s, 1, j) + r.small[s, 5:6]
        r.out_low[s, j] = result.astype(LOW)
        r.hidden[j] = result.astype(LOW).astype(F32)

    def small_ready(s):
        @pl.when(a != s)
        def _():
            small_copy(0, a, s).wait_recv()

    small_ready(0)
    for j in streams:
        first_rows(j)
        enter(0, j)

    def forward(s, _):
        need(s, 0)
        need(s, 1)

        @pl.when(a != s)
        def _():
            count_copy(0, a, s).wait_recv()

        for j in streams:
            project(s, j)

            @pl.when(c == 0)
            def _():
                kv_copy(s, j).start()

            ask(s, j)
            if j == 0:

                @pl.when(c == 1)
                def _():
                    for other in streams:
                        kv_copy(s, other).wait_recv()

            attend_line(s, j)
            leave_attention(s, j)

        @pl.when(s == 0)
        def _():
            pass_all(0, (2,))
            for later in range(1, lines):
                pass_all(later, (0, 1, 2))

        @pl.when(s == 1)
        def _():
            pass_far(1, 2)
            pass_far(1, 3)
            for later in range(2, lines):
                for p in range(4):
                    pass_far(later, p)

        for j in streams:
            between(s, j)
        @pl.when(s == 0)
        def _():
            for later in range(lines):
                pass_all(later, (3,))

        need(s, 2)
        for j in streams:
            feed(s, j)
            if j == 0:
                need(s, 3)
            leave_feed(s, j)


        @pl.when(s >= 2)
        def _():
            forward_rows(s - 2)


        @pl.when(s + 1 < lines)
        def _():
            small_ready(s + 1)

        for j in streams:
            finish(s, j)

            @pl.when(s + 1 < lines)
            def _():
                enter(s + 1, j)

        home_start(out_home, s)

        @pl.when(s == 0)
        def _():
            pass_far(1, 0)
            pass_far(1, 1)

        return 0

    lax.fori_loop(0, lines, forward, 0)

    @on_owner
    def turn(s, j):
        upstream = r.upstream[j]
        r.ups[s, j, mine] = upstream
        gather_start(r.ups, s, 2, j)
        r.norm_part[s, 5:6] += column_sum(upstream)

    def feed_back(s, j):
        gather_wait(r.ups, s, 2, j)
        grad_pre = (dot_nt(r.ups[s, j], r.wp[s]) * r.slope[s, j]).astype(LOW)
        r.gpre[s, j] = grad_pre
        scatter_start(s, 2, j, dot_nt(grad_pre, r.wf[s]))
        r.norm_part[s, 6:7, :units] += column_sum(grad_pre)

    @on_owner
    def between_back(s, j):
        grad = scatter_sum(s, 2, j)
        xhat = r.xhat2[s, j]
        upstream = r.upstream[j].astype(F32)
        grad_middle = upstream + standard_back(
            grad * r.small[s, 2:3], xhat, r.inv2[s, j, :, 0:1]
        )
        r.middle[j] = grad_middle
        branch = grad_middle.astype(LOW)
        r.brn[s, j, mine] = branch
        gather_start(r.brn, s, 3, j)
        r.norm_part[s, 2:3] += column_sum(grad * xhat)
        r.norm_part[s, 3:4] += column_sum(grad)
        r.norm_part[s, 4:5] += column_sum(branch)

    def mixed_back(s, j):
        gather_wait(r.brn, s, 3, j)
        r.gmix[j] = (dot_nt(r.brn[s, j], r.wo[s]) * stream_mask(j)).astype(LOW)

    def attend_line_back(s, j):
        grad_q, grad_k, grad_v = [], [], []
        for head in range(heads):
            cols = head_cols(head)
            weights = r.soft[s, j, head]
            grad_head = r.gmix[j, :, cols]
            grad_weights = dot_nt(grad_head, r.kv[s, 1, :, cols])
            inner = jnp.sum(weights * grad_weights, axis=-1, keepdims=True)
            grad_scores = (weights * (grad_weights - inner)).astype(LOW)
            grad_k.append(scale * dot_tn(grad_scores, r.qry[s, j, :, cols]))
            grad_v.append(dot_tn(weights.astype(LOW), grad_head))
            grad_q.append(scale * dot_nn(grad_scores, r.kv[s, 0, :, cols]))
        for which, grad in enumerate((grad_k, grad_v)):
            grad = jnp.concatenate(grad, axis=-1)
            r.dkv_all[which] = grad if j == STREAMS - 1 else r.dkv_all[which] + grad
        grad_q = jnp.concatenate(grad_q, axis=-1).astype(LOW)
        r.dqkv[s, 0, j] = grad_q
        r.norm_part[s, 7:8, :head_width] += column_sum(grad_q)

    def join_keys(s, j):
        for which in range(2):
            joined = r.dkv_all[which, row_block(c * STREAMS + j, stream_rows)].astype(LOW)
            r.dqkv[s, 1 + which, j] = joined
            if which == 1:
                lanes = slice(half_width, half_width + head_width)
                r.norm_part[s, 7:8, lanes] += column_sum(joined)

    def leave_back(s, j):
        product = dot_nn(r.dqkv[s, 0, j], r.wq[s, 0:head_width])
        for which in range(1, 3):
            weight = r.wq[s, which * head_width : (which + 1) * head_width]
            product = product + dot_nn(r.dqkv[s, which, j], weight)
        scatter_start(s, 3, j, product)

    @on_owner
    def finish_back(s, j):
        grad = scatter_sum(s, 3, j)
        xhat = r.xhat1[s, j]
        result = r.middle[j] + standard_back(
            grad * r.small[s, 0:1], xhat, r.inv1[s, j, :, 0:1]
        )
        r.upstream[j] = result.astype(LOW)
        r.grad_low[s, j] = result.astype(LOW)
        r.norm_part[s, 0:1] += column_sum(grad * xhat)
        r.norm_part[s, 1:2] += column_sum(grad)

    last_first = tuple(reversed(streams))
    for j in last_first:
        turn(lines - 1, j)

    def backward(index, _):
        s = lines - 1 - index
        for j in last_first:
            feed_back(s, j)
        rows_start(UPS, s)
        rows_start(GPRE, s)

        @pl.when(index < 2)
        def _():
            forward_rows(lines - 2 + index)

        @pl.when(index == lines - 1)
        def _():
            share(ACT)
            share(MIX)

        for j in last_first:
            between_back(s, j)
        for j in last_first:
            mixed_back(s, j)
            if j == 0:
                rows_start(BRN, s)
            attend_line_back(s, j)

            @pl.when(c == 1)
            def _():
                join_keys(s, j)
                leave_back(s, j)

        @pl.when(c == 1)
        def _():
            r.dkv_out[s] = r.dkv_all[:, 0:local].astype(LOW)
            dkv_copy(s).start()

        @pl.when(c == 0)
        def _():
            dkv_copy(s).wait_recv()
            r.dkv_all[:, 0:local] += r.dkv_in[s].astype(F32)
            for j in last_first:
                join_keys(s, j)
                leave_back(s, j)

        rows_start(DQKV, s)

        @pl.when(s == 0)
        def _():
            pass_rows(UPS)
            pass_rows(GPRE)

        for j in last_first:
            finish_back(s, j)

            @pl.when(s > 0)
            def _():
                turn(s - 1, j)

        norm_start(s)
        home_start(grad_home, s)
        return 0

    lax.fori_loop(0, lines, backward, 0)

    share(GPRE)
    for line in range(lines):
        drain(r.all_dqkv.at[line, c], r.heads_r.at[line])
        share_heads(line, c).start()

    drain(r.norm_all, r.norm_r)
    slot = c * chips + t
    norm_sum = r.norm_all[0]
    for line in range(1, lines):
        norm_sum = norm_sum + r.norm_all[line]
    r.ends[slot] = norm_sum

    def ends_copy(step):
        core, chip = step // chips, step % chips
        view = r.ends.at[slot]
        return remote(
            view,
            view,
            r.ends_s.at[step - 1],
            r.ends_r,
            seq=(c + core) % 2,
            tensor=(t + chip) % chips,
        )

    for step in range(1, 2 * chips):
        ends_copy(step).start()

    for index in (UPS, GPRE):

        @pl.when(a == 3)
        def _():
            detour_copy(index).wait_send()

        @pl.when(a == 1)
        def _():
            for copy in passed_copies(index):
                copy.wait_send()

    for kind, buffer in enumerate((r.nrm, r.nmlp, r.ups, r.brn)):
        for j in streams:
            scatter_sent(0, kind, j)

            @pl.when(middle_chip)
            def _():
                gather_sent(buffer, 0, kind, j)

    for index in range(ACT):
        drain(all_rows[index], r.rows_r.at[index])
    for index in range(ACT, DQKV):
        share_copy(index, 1 - c).wait_recv()
        share_copy(index, c).wait_send()
    for line in range(lines):
        share_heads(line, 1 - c).wait_recv()
        share_heads(line, c).wait_send()
    drain(r.acts, r.out_r)
    drain(r.grads, r.grad_r)
    drain(r.ends.at[0 : 2 * chips - 1], r.ends_r)
    for step in range(1, 2 * chips):
        ends_copy(step).wait_send()
    for step in range(1, lines):
        small_copy(step - 1, (a + step) % lines, a).wait_send()
        count_copy(step - 1, (a + step) % lines, a).wait_send()
    for p in range(4):
        for which, line in enumerate((beside(a), above(a))):
            first_hop(p, a, line, which).wait_send()

    first_copy(t // 2).wait_send()

    def sent(s, _):
        home_sent(out_home, s)
        home_sent(grad_home, s)

        @pl.when(a != s)
        def _():
            norm_copy(s).wait_send()

        @pl.when(c == 0)
        def _():
            for j in streams:
                kv_copy(s, j).wait_send()

        @pl.when(c == 1)
        def _():
            dkv_copy(s).wait_send()

        for index in range(8):
            rows_sent(index, s)
        for p in range(4):

            @pl.when((a == beside(s)) | (a == above(s)))
            def _():
                second_hop(p, s, 0).wait_send()

            @pl.when(a != s)
            def _():
                core_hop(p, s, c).wait_send()

        return 0

    lax.fori_loop(0, lines, sent, 0)


def relay_call(inputs, cotangent, lengths, chosen, singles, weights):
    lines = lax.axis_size("section")
    chips = lax.axis_size("tensor")
    rows, buckets, width = inputs.shape[1:]
    local, total, half = rows * chips, 2 * rows * chips, width // 2
    head_width, units = weights["wo_in"].shape[0], weights["wp_in"].shape[0]
    heads = head_width // HDIM
    stream = local // STREAMS
    peers, owned = chips - 1, stream // 2
    vmem, dma = pltpu.VMEM, pltpu.SemaphoreType.DMA
    operands = dict(
        inputs=inputs,
        cotangent=cotangent,
        lengths=lengths,
        chosen=chosen,
        **singles,
        **weights,
    )

    def space(name):
        if name in weights:
            return pl.ANY
        return pltpu.SMEM if operands[name] is lengths else pltpu.VMEM

    sums = dict(
        acts=((lines, rows, width), LOW),
        grads=((lines, rows, width), LOW),
        ends=((2 * chips, 8, width), F32),
    )
    gathered = dict(
        all_nrm=((lines, 2, STREAMS, stream, half), LOW),
        all_nmlp=((lines, 2, STREAMS, stream, half), LOW),
        all_ups=((lines, 2, STREAMS, stream, half), LOW),
        all_brn=((lines, 2, STREAMS, stream, half), LOW),
        all_act=((lines, 2, STREAMS, stream, units), LOW),
        all_gpre=((lines, 2, STREAMS, stream, units), LOW),
        all_mix=((lines, 2, STREAMS, stream, head_width), LOW),
        all_dqkv=((lines, 2, 3, STREAMS, stream, head_width), LOW),
    )
    outputs = dict(**sums, **gathered)
    scratch = dict(
        wq=vmem((lines,) + weights["wq_in"].shape, LOW),
        wo=vmem((lines,) + weights["wo_in"].shape, LOW),
        wf=vmem((lines,) + weights["wf_in"].shape, LOW),
        wp=vmem((lines,) + weights["wp_in"].shape, LOW),
        small_own=vmem((8, width), F32),
        small=vmem((lines, 8, width), F32),
        count_own=vmem((lines, 8, total), F32),
        count=vmem((lines, 8, total), F32),
        hidden=vmem((STREAMS, owned, width), F32),
        middle=vmem((STREAMS, owned, width), F32),
        upstream=vmem((STREAMS, owned, width), LOW),
        first_out=vmem((2, owned, width), LOW),
        first_in=vmem((STREAMS, 2, owned, width), LOW),
        xhat1=vmem((lines, STREAMS, owned, width), F32),
        inv1=vmem((lines, STREAMS, owned, 128), F32),
        xhat2=vmem((lines, STREAMS, owned, width), F32),
        inv2=vmem((lines, STREAMS, owned, 128), F32),
        nrm=vmem((lines, STREAMS, stream, width), LOW),
        nmlp=vmem((lines, STREAMS, stream, width), LOW),
        ups=vmem((lines, STREAMS, stream, width), LOW),
        brn=vmem((lines, STREAMS, stream, width), LOW),
        act=vmem((lines, STREAMS, stream, units), LOW),
        gpre=vmem((lines, STREAMS, stream, units), LOW),
        slope=vmem((lines, STREAMS, stream, units), F32),
        mix=vmem((lines, STREAMS, stream, head_width), LOW),
        qry=vmem((lines, STREAMS, stream, head_width), LOW),
        gmix=vmem((STREAMS, stream, head_width), LOW),
        dqkv=vmem((lines, 3, STREAMS, stream, head_width), LOW),
        pass_ups=vmem((STREAMS, stream, width), LOW),
        pass_gpre=vmem((STREAMS, stream, units), LOW),
        kv=vmem((lines, 2, total, head_width), LOW),
        soft=vmem((lines, STREAMS, heads, stream, total), F32),
        near=vmem((STREAMS, stream, total), F32),
        dkv_all=vmem((2, total, head_width), F32),
        dkv_out=vmem((lines, 2, local, head_width), LOW),
        dkv_in=vmem((lines, 2, local, head_width), LOW),
        part=vmem((4, STREAMS, stream, width), LOW),
        arrived=vmem((lines, 4, STREAMS, peers, owned, width), LOW),
        out_low=vmem((lines, STREAMS, owned, width), LOW),
        grad_low=vmem((lines, STREAMS, owned, width), LOW),
        norm_part=vmem((lines, 8, width), F32),
        norm_all=vmem((lines, 8, width), F32),
        w_first_s=dma((4, 2)),
        w_first_r=dma((lines, 4)),
        w_second_s=dma((lines, 4)),
        w_second_r=dma((lines, 4, 2)),
        w_core_s=dma((lines, 4)),
        w_core_r=dma((lines, 4)),
        w_own=dma((4,)),
        small_s=dma((lines - 1,)),
        small_r=dma((lines,)),
        count_s=dma((lines - 1,)),
        count_r=dma((lines,)),
        ag_s=dma((4, STREAMS, peers)),
        ag_r=dma((4, STREAMS, peers)),
        rs_s=dma((4, STREAMS, peers)),
        rs_r=dma((4, STREAMS, peers)),
        kv_s=dma((lines, STREAMS)),
        kv_r=dma((lines, STREAMS)),
        dkv_s=dma((lines,)),
        dkv_r=dma((lines,)),
        rows_s=dma((8, lines, 2)),
        rows_r=dma((8,)),
        pass_s=dma((2,)),
        pass_r=dma((2,)),
        pass_on_s=dma((2, 2)),
        share_s=dma((4,)),
        share_r=dma((4,)),
        heads_r=dma((lines,)),
        heads_s=dma((lines,)),
        heads_sr=dma((lines,)),
        first_s=dma,
        first_r=dma((STREAMS,)),
        out_s=dma((lines, STREAMS)),
        out_r=dma,
        grad_s=dma((lines, STREAMS)),
        grad_r=dma,
        norm_s=dma((lines,)),
        norm_r=dma,
        ends_s=dma((2 * chips - 1,)),
        ends_r=dma,
    )
    names = tuple(operands) + tuple(outputs) + tuple(scratch)
    apart = ("all_nrm", "all_nmlp", "all_ups", "all_brn")
    results = pl.pallas_call(
        functools.partial(relay_kernel, names),
        out_shape=[jax.ShapeDtypeStruct(shape, kind) for shape, kind in outputs.values()],
        in_specs=[pl.BlockSpec(memory_space=space(name)) for name in operands],
        out_specs=[
            pl.BlockSpec(memory_space=pl.ANY if name in apart else pltpu.VMEM)
            for name in outputs
        ],
        scratch_shapes=list(scratch.values()),
        compiler_params=pltpu.CompilerParams(
            collective_id=0, has_side_effects=True, vmem_limit_bytes=60 * 2**20
        ),
        name="relay",
    )(*operands.values())
    return dict(zip(outputs, results))


def weights_kernel(names, *refs):
    r = types.SimpleNamespace(**dict(zip(names, refs)))
    micro_count, rows, buckets, width = r.activations.shape
    chips, units, head_width = r.ends.shape[0] // 2, r.all_act.shape[-1], r.all_mix.shape[-1]
    lines = r.acts.shape[0]
    loads = [
        pltpu.make_async_copy(source, target, r.load_sem.at[place])
        for place, (source, target) in enumerate(
            (
                (r.all_act, r.act),
                (r.all_ups, r.ups),
                (r.all_nmlp, r.nmlp),
                (r.all_gpre, r.gpre),
                (r.all_mix, r.mix),
                (r.all_brn, r.brn),
                (r.all_nrm, r.nrm),
                (r.all_dqkv, r.dqkv),
            )
        )
    ]
    stores = [
        pltpu.make_async_copy(source, target, r.store_sem.at[place])
        for place, (source, target) in enumerate(
            (
                (r.own_proj, r.w_proj),
                (r.own_fc, r.w_fc),
                (r.own_out, r.w_out),
                (r.own_qkv, r.w_qkv),
            )
        )
    ]
    for load in loads:
        load.start()

    sums = r.ends[0]
    for other in range(1, 2 * chips):
        sums = sums + r.ends[other]
    singles = (r.ln1_gain, r.ln1_shift, r.ln2_gain, r.ln2_shift, r.b_out, r.b_proj)
    for place, single in enumerate(singles):
        single[...] = sums[place : place + 1]
    for chip in range(chips):
        both = r.ends[chip] + r.ends[chips + chip]
        r.b_fc[:, chip * units : (chip + 1) * units] = both[6:7, :units]
        here = slice(chip * head_width, (chip + 1) * head_width)
        r.b_qv[0:1, here] = both[7:8, :head_width]
        r.b_qv[1:2, here] = both[7:8, width // 2 : width // 2 + head_width]
    for target, source in ((r.activations, r.acts), (r.in_grads, r.grads)):
        for micro in range(micro_count):
            rows_of = [
                source[micro * buckets + bucket].astype(F32)[:, None, :]
                for bucket in range(buckets)
            ]
            target[micro] = jnp.concatenate(rows_of, axis=1).astype(LOW)

    def flat(array):
        return array.reshape(lines * 2 * chips * rows, array.shape[-1])

    loads[0].wait()
    loads[1].wait()
    r.own_proj[...] = dot_tn(flat(r.act[...]), flat(r.ups[...]))
    stores[0].start()
    loads[2].wait()
    loads[3].wait()
    r.own_fc[...] = dot_tn(flat(r.nmlp[...]), flat(r.gpre[...]))
    stores[1].start()
    loads[4].wait()
    loads[5].wait()
    r.own_out[...] = dot_tn(flat(r.mix[...]), flat(r.brn[...]))
    stores[2].start()
    loads[6].wait()
    loads[7].wait()
    nrm = flat(r.nrm[...])
    for which in range(3):
        r.own_qkv[which] = dot_tn(flat(r.dqkv[:, :, which]), nrm)
    stores[3].start()
    for store in stores:
        store.wait()


def weights_call(relayed, inputs_shape, head_width, units):
    chips = lax.axis_size("tensor")
    width = inputs_shape[-1]
    half = width // 2
    outputs = dict(
        activations=(inputs_shape, LOW),
        in_grads=(inputs_shape, LOW),
        ln1_gain=((1, width), F32),
        ln1_shift=((1, width), F32),
        w_qkv=((3, head_width, half), F32),
        b_qv=((2, width), F32),
        w_out=((head_width, half), F32),
        b_out=((1, width), F32),
        ln2_gain=((1, width), F32),
        ln2_shift=((1, width), F32),
        w_fc=((half, units), F32),
        b_fc=((1, chips * units), F32),
        w_proj=((units, half), F32),
        b_proj=((1, width), F32),
    )
    rows = ("act", "ups", "nmlp", "gpre", "mix", "brn", "nrm", "dqkv")
    own = dict(own_proj="w_proj", own_fc="w_fc", own_out="w_out", own_qkv="w_qkv")
    scratch = {name: pltpu.VMEM(relayed["all_" + name].shape, LOW) for name in rows}
    scratch.update({name: pltpu.VMEM(outputs[of][0], F32) for name, of in own.items()})
    scratch["load_sem"] = pltpu.SemaphoreType.DMA((8,))
    scratch["store_sem"] = pltpu.SemaphoreType.DMA((4,))
    whole, apart = pl.BlockSpec(memory_space=pltpu.VMEM), pl.BlockSpec(memory_space=pl.ANY)
    small = ("acts", "grads", "ends")
    return pl.pallas_call(
        functools.partial(weights_kernel, tuple(relayed) + tuple(outputs) + tuple(scratch)),
        out_shape=[jax.ShapeDtypeStruct(shape, kind) for shape, kind in outputs.values()],
        in_specs=[whole if name in small else apart for name in relayed],
        out_specs=[apart if name in own.values() else whole for name in outputs],
        scratch_shapes=list(scratch.values()),
        compiler_params=pltpu.CompilerParams(vmem_limit_bytes=60 * 2**20),
        name="weight_gradients",
    )(*relayed.values())


def on_line(
    inputs,
    cotangent,
    lengths,
    chosen,
    ln1_gain,
    ln1_shift,
    w_qkv,
    b_qv,
    w_out,
    b_out,
    ln2_gain,
    ln2_shift,
    w_fc,
    b_fc,
    w_proj,
    b_proj,
):
    head_width, units = w_out.shape[1], w_fc.shape[2]
    singles = dict(
        ln1_gain=ln1_gain,
        ln1_shift=ln1_shift,
        ln2_gain=ln2_gain,
        ln2_shift=ln2_shift,
        b_out=b_out,
        b_proj=b_proj,
        b_fc=b_fc,
        b_qv=b_qv[0],
    )
    weights = dict(
        wq_in=jnp.swapaxes(w_qkv[0], 1, 2).reshape(-1, inputs.shape[-1]),
        wo_in=w_out[0],
        wf_in=w_fc[0],
        wp_in=w_proj[0],
    )
    picks = chosen.reshape((-1,) + chosen.shape[-2:])
    relayed = relay_call(inputs, cotangent, lengths, picks, singles, weights)
    results = list(weights_call(relayed, inputs.shape, head_width, units))
    results[4] = jnp.swapaxes(results[4], 1, 2)
    vectors = (2, 3, 7, 8, 9, 11, 13)
    return tuple(
        result if place in vectors else result[None] for place, result in enumerate(results)
    )


def fits_lines(mesh):
    return mesh.shape["section"] == 4 and mesh.shape["seq"] == 2 and mesh.shape["tensor"] == 4


def solution(mesh):
    placed = (
        P(None, ("seq", "tensor"), None, None),
        P(None, ("seq", "tensor"), None, None),
        P(),
        P("section", None, None, "tensor", "seq", None),
        P("section", None),
        P("section", None),
        P("section", None, None, "tensor"),
        P("section", None, "tensor"),
        P("section", "tensor", None),
        P("section", None),
        P("section", None),
        P("section", None),
        P("section", None, "tensor"),
        P("section", "tensor"),
        P("section", "tensor", None),
        P("section", None),
    )
    return jax.shard_map(
        on_line if fits_lines(mesh) else on_device,
        mesh=mesh,
        in_specs=placed,
        out_specs=(
            P("section", None, ("seq", "tensor"), None, None),
            P("section", None, ("seq", "tensor"), None, None),
            P("section", None),
            P("section", None),
            P("section", None, "seq", "tensor"),
            P("section", None, None),
            P("section", "tensor", "seq"),
            P("section", None),
            P("section", None),
            P("section", None),
            P("section", "seq", "tensor"),
            P("section", None),
            P("section", "tensor", "seq"),
            P("section", None),
        ),
        check_vma=False,
    )
```

```python
import functools
import types

import jax
import jax.numpy as jnp
from jax import lax
from jax.experimental import pallas as pl
from jax.experimental.pallas import tpu as pltpu
from jax.sharding import PartitionSpec as P

HDIM = 64
WIN = 64
QB = 64
KSEL = 64


NORM_EPS = 1e-05
MASKED = -1000000000.0


def from_behind(value, axis, steps):
    count = lax.axis_size(axis)
    first, last = (max(0, -steps), min(count, count - steps))
    return lax.ppermute(value, axis, [(source, source + steps) for source in range(first, last)])


def layer_norm(values, gain, shift):
    average = jnp.mean(values, axis=-1, keepdims=True)
    centred = values - average
    variance = jnp.mean(centred * centred, axis=-1, keepdims=True)
    return centred * lax.rsqrt(variance + NORM_EPS) * gain + shift


def gelu_tanh(values):
    return (
        0.5
        * values
        * (1.0 + jnp.tanh(0.7978845608028654 * (values + 0.044715 * values * values * values)))
    )


def gather_rows(row_block):
    return lax.all_gather(row_block, "tensor", axis=0, tiled=True)


def scatter_product(left_rows, weight, formula):
    return lax.psum_scatter(
        jnp.einsum(formula, left_rows, weight, preferred_element_type=jnp.float32).astype(
            jnp.bfloat16
        ),
        "tensor",
        scatter_dimension=0,
        tiled=True,
    ).astype(jnp.float32)


def near_slabs(full_rows, seq_start, seq_first, length_local):
    buckets = full_rows.shape[1]
    heads_local = full_rows.shape[2] // HDIM
    blocks = length_local // QB
    earlier = lax.dynamic_slice_in_dim(full_rows, jnp.maximum(seq_start - WIN, 0), WIN, 0)
    earlier = jnp.where(seq_first, jnp.zeros_like(earlier), earlier)
    local_part = lax.dynamic_slice_in_dim(full_rows, seq_start, length_local, 0)
    segment = jnp.concatenate([earlier, local_part], 0).reshape(
        length_local + WIN, buckets, heads_local, HDIM
    )
    return jnp.concatenate(
        [
            segment[offset_index * QB : offset_index * QB + length_local].reshape(
                blocks, QB, buckets, heads_local, HDIM
            )
            for offset_index in range(WIN // QB + 1)
        ],
        1,
    )


def far_rows(full_rows, flat_index):
    total_rows, buckets, feature_width = full_rows.shape
    heads_local = feature_width // HDIM
    return jnp.take(full_rows.reshape(total_rows * buckets * heads_local, HDIM), flat_index, axis=0)


def key_geometry(chosen_now, seq_start, blocks):
    buckets, heads_local = (chosen_now.shape[0], chosen_now.shape[1])
    bucket_ids = lax.broadcasted_iota(jnp.int32, chosen_now.shape, 0)
    head_ids = lax.broadcasted_iota(jnp.int32, chosen_now.shape, 1)
    flat_index = (chosen_now * buckets + bucket_ids) * heads_local + head_ids
    block_start = seq_start + QB * lax.broadcasted_iota(jnp.int32, (blocks, 1, 1), 0)
    query_ids = lax.broadcasted_iota(jnp.int32, (1, QB, 1), 1)
    key_ids = lax.broadcasted_iota(jnp.int32, (1, 1, WIN + QB), 2)
    distance = query_ids + WIN - key_ids
    near_ok = (distance >= 0) & (distance < WIN) & (block_start + key_ids - WIN >= 0)
    far_ok = chosen_now + WIN <= block_start.reshape(1, 1, blocks, 1)
    near_mask = jnp.broadcast_to(
        near_ok[:, None, None], (blocks, buckets, heads_local, QB, WIN + QB)
    )
    far_mask = jnp.broadcast_to(
        jnp.transpose(far_ok, (2, 0, 1, 3))[:, :, :, None, :],
        (blocks, buckets, heads_local, QB, KSEL),
    )
    return (flat_index, jnp.concatenate([near_mask, far_mask], -1))


def attention_setup(queries, key_rows, value_rows, chosen_now, seq_start, seq_first):
    length_local, buckets, feature_width = queries.shape
    heads_local = feature_width // HDIM
    blocks = length_local // QB
    query_blocks = queries.reshape(blocks, QB, buckets, heads_local, HDIM)
    flat_index, key_mask = key_geometry(chosen_now, seq_start, blocks)
    near_keys = near_slabs(key_rows, seq_start, seq_first, length_local)
    near_values = near_slabs(value_rows, seq_start, seq_first, length_local)
    far_keys = far_rows(key_rows, flat_index)
    far_values = far_rows(value_rows, flat_index)
    near_scores = jnp.einsum(
        "bqnhe,btnhe->bnhqt", query_blocks, near_keys, preferred_element_type=jnp.float32
    )
    far_scores = jnp.einsum(
        "bqnhe,nhbke->bnhqk", query_blocks, far_keys, preferred_element_type=jnp.float32
    )
    scores = jnp.where(
        key_mask, HDIM ** (-0.5) * jnp.concatenate([near_scores, far_scores], -1), MASKED
    )
    return (query_blocks, near_keys, near_values, far_keys, far_values, flat_index, scores)


def attend(queries, key_rows, value_rows, chosen_now, seq_start, seq_first):
    query_blocks, near_keys, near_values, far_keys, far_values, flat_index, scores = (
        attention_setup(queries, key_rows, value_rows, chosen_now, seq_start, seq_first)
    )
    span = WIN + QB
    row_top = jnp.max(scores, -1, keepdims=True)
    exp_terms = jnp.exp(scores - row_top)
    row_total = jnp.sum(exp_terms, -1, keepdims=True)
    softmax_low = (exp_terms / row_total).astype(jnp.bfloat16)
    near_part = jnp.einsum(
        "bnhqt,btnhe->bqnhe",
        softmax_low[..., :span],
        near_values,
        preferred_element_type=jnp.float32,
    )
    far_part = jnp.einsum(
        "bnhqk,nhbke->bqnhe",
        softmax_low[..., span:],
        far_values,
        preferred_element_type=jnp.float32,
    )
    return ((near_part + far_part).reshape(queries.shape), row_top + jnp.log(row_total))


def spread_back(near_grad, far_grad, flat_index, seq_start, seq_first, total_rows):
    blocks, span, buckets, heads_local, head_size = near_grad.shape
    length_local = blocks * QB
    feature_width = heads_local * head_size
    segment = jnp.zeros((length_local + WIN, buckets, heads_local, head_size), jnp.float32)
    for offset_index in range(WIN // QB + 1):
        piece = near_grad[:, offset_index * QB : (offset_index + 1) * QB].reshape(
            length_local, buckets, heads_local, head_size
        )
        segment = segment.at[offset_index * QB : offset_index * QB + length_local].add(piece)
    full_rows = jnp.zeros((total_rows * buckets * heads_local, head_size), jnp.float32)
    full_rows = full_rows.at[flat_index.reshape(-1)].add(far_grad.reshape(-1, head_size))
    full_rows = full_rows.reshape(total_rows, buckets, feature_width)
    local_part = segment[WIN:].reshape(length_local, buckets, feature_width)
    earlier = jnp.where(seq_first, 0.0, segment[:WIN].reshape(WIN, buckets, feature_width))
    full_rows = lax.dynamic_update_slice_in_dim(
        full_rows,
        lax.dynamic_slice_in_dim(full_rows, seq_start, length_local, 0) + local_part,
        seq_start,
        0,
    )
    earlier_start = jnp.maximum(seq_start - WIN, 0)
    full_rows = lax.dynamic_update_slice_in_dim(
        full_rows,
        lax.dynamic_slice_in_dim(full_rows, earlier_start, WIN, 0) + earlier,
        earlier_start,
        0,
    )
    return full_rows


def attend_back(
    queries, key_rows, value_rows, chosen_now, seq_start, seq_first, log_total, grad_mixed
):
    query_blocks, near_keys, near_values, far_keys, far_values, flat_index, scores = (
        attention_setup(queries, key_rows, value_rows, chosen_now, seq_start, seq_first)
    )
    span = WIN + QB
    score_scale = HDIM ** (-0.5)
    grad_blocks = grad_mixed.reshape(query_blocks.shape)
    weights_full = jnp.exp(scores - log_total)
    softmax_low = weights_full.astype(jnp.bfloat16)
    grad_near_weights = jnp.einsum(
        "bqnhe,btnhe->bnhqt", grad_blocks, near_values, preferred_element_type=jnp.float32
    )
    grad_far_weights = jnp.einsum(
        "bqnhe,nhbke->bnhqk", grad_blocks, far_values, preferred_element_type=jnp.float32
    )
    grad_weights = jnp.concatenate([grad_near_weights, grad_far_weights], -1)
    row_dot = jnp.sum(weights_full * grad_weights, -1, keepdims=True)
    grad_scores = (weights_full * (grad_weights - row_dot)).astype(jnp.bfloat16)
    grad_near, grad_far = (grad_scores[..., :span], grad_scores[..., span:])
    grad_queries = score_scale * (
        jnp.einsum("bnhqt,btnhe->bqnhe", grad_near, near_keys, preferred_element_type=jnp.float32)
        + jnp.einsum("bnhqk,nhbke->bqnhe", grad_far, far_keys, preferred_element_type=jnp.float32)
    )
    near_key_grad = score_scale * jnp.einsum(
        "bnhqt,bqnhe->btnhe", grad_near, query_blocks, preferred_element_type=jnp.float32
    )
    far_key_grad = score_scale * jnp.einsum(
        "bnhqk,bqnhe->nhbke", grad_far, query_blocks, preferred_element_type=jnp.float32
    )
    near_value_grad = jnp.einsum(
        "bnhqt,bqnhe->btnhe",
        softmax_low[..., :span],
        grad_blocks,
        preferred_element_type=jnp.float32,
    )
    far_value_grad = jnp.einsum(
        "bnhqk,bqnhe->nhbke",
        softmax_low[..., span:],
        grad_blocks,
        preferred_element_type=jnp.float32,
    )
    total_rows = key_rows.shape[0]
    key_grad = spread_back(
        near_key_grad, far_key_grad, flat_index, seq_start, seq_first, total_rows
    )
    value_grad = spread_back(
        near_value_grad, far_value_grad, flat_index, seq_start, seq_first, total_rows
    )
    return (grad_queries.reshape(queries.shape), key_grad, value_grad)


def forward_pass(hidden, params, chosen_now, query_mask, seq_start, seq_first, finish):
    (
        ln1_gain,
        ln1_shift,
        w_qkv,
        b_qv,
        w_out,
        b_out,
        ln2_gain,
        ln2_shift,
        w_fc,
        b_fc,
        w_proj,
        b_proj,
    ) = params
    hidden_wide = hidden.astype(jnp.float32)
    normed_all = gather_rows(layer_norm(hidden_wide, ln1_gain, ln1_shift).astype(jnp.bfloat16))
    projected = jnp.einsum("pnd,jdc->jpnc", normed_all, w_qkv, preferred_element_type=jnp.float32)
    queries = (projected[0] + b_qv[0]).astype(jnp.bfloat16)
    key_rows, value_rows = (
        lax.all_gather(projected[1].astype(jnp.bfloat16), "seq", axis=0, tiled=True),
        lax.all_gather((projected[2] + b_qv[1]).astype(jnp.bfloat16), "seq", axis=0, tiled=True),
    )
    attended, log_total = attend(queries, key_rows, value_rows, chosen_now, seq_start, seq_first)
    mixed_rows = (attended * query_mask[:, :, None]).astype(jnp.bfloat16)
    middle = hidden_wide + scatter_product(mixed_rows, w_out, "pnc,cd->pnd") + b_out
    normed_mlp = gather_rows(layer_norm(middle, ln2_gain, ln2_shift).astype(jnp.bfloat16))
    pre_active = (
        jnp.einsum("pnd,df->pnf", normed_mlp, w_fc, preferred_element_type=jnp.float32) + b_fc
    )
    active = gelu_tanh(pre_active).astype(jnp.bfloat16)
    if not finish:
        return (
            normed_all,
            queries,
            key_rows,
            value_rows,
            log_total,
            mixed_rows,
            middle,
            normed_mlp,
            pre_active,
            active,
        )
    output = (middle + scatter_product(active, w_proj, "pnf,fd->pnd") + b_proj).astype(jnp.bfloat16)
    return (output, (key_rows, value_rows))


def backward_pass(hidden, upstream, params, chosen_now, query_mask, seq_start, seq_first):
    (
        ln1_gain,
        ln1_shift,
        w_qkv,
        b_qv,
        w_out,
        b_out,
        ln2_gain,
        ln2_shift,
        w_fc,
        b_fc,
        w_proj,
        b_proj,
    ) = params
    (
        normed_all,
        queries,
        key_rows,
        value_rows,
        log_total,
        mixed_rows,
        middle,
        normed_mlp,
        pre_active,
        active,
    ) = forward_pass(hidden, params, chosen_now, query_mask, seq_start, seq_first, False)
    upstream_all = gather_rows(upstream)
    grad_w_proj = jnp.einsum(
        "pnf,pnd->fd", active, upstream_all, preferred_element_type=jnp.float32
    )
    grad_b_proj = jnp.sum(upstream.astype(jnp.float32), axis=(0, 1))
    grad_active = jnp.einsum(
        "pnd,fd->pnf", upstream_all, w_proj, preferred_element_type=jnp.float32
    )
    unused_value, gelu_pull = jax.vjp(gelu_tanh, pre_active)
    grad_pre = gelu_pull(grad_active)[0].astype(jnp.bfloat16)
    grad_w_fc = jnp.einsum("pnd,pnf->df", normed_mlp, grad_pre, preferred_element_type=jnp.float32)
    grad_b_fc = jnp.sum(grad_pre.astype(jnp.float32), axis=(0, 1))
    grad_normed_mlp = scatter_product(grad_pre, w_fc, "pnf,df->pnd")
    unused_norm, second_pull = jax.vjp(layer_norm, middle, ln2_gain, ln2_shift)
    grad_mid_norm, grad_ln2_gain, grad_ln2_shift = second_pull(grad_normed_mlp)
    grad_middle = upstream.astype(jnp.float32) + grad_mid_norm
    grad_branch = grad_middle.astype(jnp.bfloat16)
    grad_b_out = jnp.sum(grad_branch.astype(jnp.float32), axis=(0, 1))
    branch_all = gather_rows(grad_branch)
    grad_w_out = jnp.einsum(
        "pnc,pnd->cd", mixed_rows, branch_all, preferred_element_type=jnp.float32
    )
    grad_mixed = jnp.einsum(
        "pnd,cd->pnc", branch_all, w_out, preferred_element_type=jnp.float32
    ).astype(jnp.bfloat16) * query_mask[:, :, None].astype(jnp.bfloat16)
    grad_queries, key_grad_all, value_grad_all = attend_back(
        queries, key_rows, value_rows, chosen_now, seq_start, seq_first, log_total, grad_mixed
    )
    key_grad, value_grad = (
        lax.psum_scatter(
            key_grad_all.astype(jnp.bfloat16), "seq", scatter_dimension=0, tiled=True
        ).astype(jnp.float32),
        lax.psum_scatter(
            value_grad_all.astype(jnp.bfloat16), "seq", scatter_dimension=0, tiled=True
        ).astype(jnp.float32),
    )
    grad_project = jnp.stack(
        [
            grad_queries.astype(jnp.bfloat16),
            key_grad.astype(jnp.bfloat16),
            value_grad.astype(jnp.bfloat16),
        ],
        2,
    )
    grad_w_qkv = jnp.einsum(
        "pnd,pnjc->jdc", normed_all, grad_project, preferred_element_type=jnp.float32
    )
    grad_b_qv = jnp.sum(grad_project[:, :, 0::2].astype(jnp.float32), axis=(0, 1))
    grad_normed = scatter_product(grad_project, w_qkv, "pnjc,jdc->pnd")
    unused_first, first_pull = jax.vjp(layer_norm, hidden.astype(jnp.float32), ln1_gain, ln1_shift)
    grad_in_norm, grad_ln1_gain, grad_ln1_shift = first_pull(grad_normed)
    grad_hidden = (grad_middle + grad_in_norm).astype(jnp.bfloat16)
    block_grads = (
        grad_ln1_gain,
        grad_ln1_shift,
        grad_w_qkv,
        grad_b_qv,
        grad_w_out,
        grad_b_out,
        grad_ln2_gain,
        grad_ln2_shift,
        grad_w_fc,
        grad_b_fc,
        grad_w_proj,
        grad_b_proj,
    )
    return (grad_hidden, block_grads)


def on_device(
    inputs,
    cotangent,
    lengths,
    chosen,
    ln1_gain,
    ln1_shift,
    w_qkv,
    b_qv,
    w_out,
    b_out,
    ln2_gain,
    ln2_shift,
    w_fc,
    b_fc,
    w_proj,
    b_proj,
):
    params = tuple(
        (
            weight_array[0]
            for weight_array in (
                ln1_gain,
                ln1_shift,
                w_qkv,
                b_qv,
                w_out,
                b_out,
                ln2_gain,
                ln2_shift,
                w_fc,
                b_fc,
                w_proj,
                b_proj,
            )
        )
    )
    section_index = lax.axis_index("section")
    section_count = lax.axis_size("section")
    seq_index = lax.axis_index("seq")
    tensor_index = lax.axis_index("tensor")
    tensor_count = lax.axis_size("tensor")
    micro_count, rows_local, buckets, feature_width = inputs.shape
    length_local = rows_local * tensor_count
    heads_width = w_qkv.shape[-1]
    seq_start = seq_index * length_local
    seq_first = seq_index == 0
    positions = seq_start + lax.broadcasted_iota(jnp.int32, (micro_count, length_local, buckets), 1)
    mask_all = (positions < lengths[:, None, :]).astype(jnp.float32)
    mask_rows = lax.dynamic_slice_in_dim(mask_all, tensor_index * rows_local, rows_local, 1)
    step_count = micro_count + section_count - 1
    chosen_section = chosen[0]
    received = jnp.zeros((rows_local, buckets, feature_width), jnp.bfloat16)
    stored = jnp.zeros((micro_count, rows_local, buckets, feature_width), jnp.bfloat16)
    outputs = jnp.zeros_like(stored)
    for step_index in range(step_count):
        micro_index = step_index - section_index
        running = (micro_index >= 0) & (micro_index < micro_count)
        slot_index = jnp.clip(micro_index, 0, micro_count - 1)
        block_in = jnp.where(
            section_index == 0, lax.dynamic_index_in_dim(inputs, slot_index, 0, False), received
        )
        chosen_now = lax.dynamic_index_in_dim(chosen_section, slot_index, 0, False)
        query_mask = lax.dynamic_index_in_dim(mask_all, slot_index, 0, False)
        result, key_pair = forward_pass(
            block_in, params, chosen_now, query_mask, seq_start, seq_first, True
        )
        stored = jnp.where(
            running, lax.dynamic_update_index_in_dim(stored, block_in, slot_index, 0), stored
        )
        outputs = jnp.where(
            running, lax.dynamic_update_index_in_dim(outputs, result, slot_index, 0), outputs
        )
        received = from_behind(result, "section", 1)
    back_received = jnp.zeros((rows_local, buckets, feature_width), jnp.bfloat16)
    in_grads = jnp.zeros_like(stored)
    totals = None
    for step_index in range(step_count):
        micro_index = step_index - (section_count - 1 - section_index)
        running = (micro_index >= 0) & (micro_index < micro_count)
        slot_index = jnp.clip(micro_index, 0, micro_count - 1)
        chosen_now = lax.dynamic_index_in_dim(chosen_section, slot_index, 0, False)
        query_mask = lax.dynamic_index_in_dim(mask_all, slot_index, 0, False)
        local_mask = lax.dynamic_index_in_dim(mask_rows, slot_index, 0, False)
        top_grad = (
            lax.dynamic_index_in_dim(cotangent, slot_index, 0, False).astype(jnp.float32)
            * local_mask[:, :, None]
        ).astype(jnp.bfloat16)
        upstream = jnp.where(section_index == section_count - 1, top_grad, back_received)
        hidden = lax.dynamic_index_in_dim(stored, slot_index, 0, False)
        grad_hidden, block_grads = backward_pass(
            hidden, upstream, params, chosen_now, query_mask, seq_start, seq_first
        )
        block_grads = tuple(
            (jnp.where(running, grad_part, jnp.zeros_like(grad_part)) for grad_part in block_grads)
        )
        totals = (
            block_grads
            if step_index == 0
            else tuple(
                (total_part + grad_part for total_part, grad_part in zip(totals, block_grads))
            )
        )
        in_grads = jnp.where(
            running, lax.dynamic_update_index_in_dim(in_grads, grad_hidden, slot_index, 0), in_grads
        )
        back_received = from_behind(grad_hidden, "section", -1)
    (
        sum_ln1_gain,
        sum_ln1_shift,
        sum_w_qkv,
        sum_b_qv,
        sum_w_out,
        sum_b_out,
        sum_ln2_gain,
        sum_ln2_shift,
        sum_w_fc,
        sum_b_fc,
        sum_w_proj,
        sum_b_proj,
    ) = totals
    part_qkv, part_out, part_fc, part_proj = (
        lax.psum_scatter(
            sum_w_qkv.astype(jnp.bfloat16), "seq", scatter_dimension=1, tiled=True
        ).astype(jnp.float32),
        lax.psum_scatter(
            sum_w_out.astype(jnp.bfloat16), "seq", scatter_dimension=1, tiled=True
        ).astype(jnp.float32),
        lax.psum_scatter(
            sum_w_fc.astype(jnp.bfloat16), "seq", scatter_dimension=0, tiled=True
        ).astype(jnp.float32),
        lax.psum_scatter(
            sum_w_proj.astype(jnp.bfloat16), "seq", scatter_dimension=1, tiled=True
        ).astype(jnp.float32),
    )
    bias_qv = lax.dynamic_update_slice_in_dim(
        jnp.zeros((2, feature_width), jnp.float32), sum_b_qv, tensor_index * heads_width, 1
    )
    units_local = sum_b_fc.shape[0]
    bias_fc = lax.dynamic_update_slice_in_dim(
        jnp.zeros((units_local * tensor_count,), jnp.float32),
        sum_b_fc,
        tensor_index * units_local,
        0,
    )
    small_sums = lax.psum(
        (
            sum_ln1_gain,
            sum_ln1_shift,
            bias_qv,
            sum_b_out,
            sum_ln2_gain,
            sum_ln2_shift,
            bias_fc,
            sum_b_proj,
        ),
        ("seq", "tensor"),
    )
    return (
        outputs[None],
        in_grads[None],
        small_sums[0][None],
        small_sums[1][None],
        part_qkv[None],
        small_sums[2][None],
        part_out[None],
        small_sums[3][None],
        small_sums[4][None],
        small_sums[5][None],
        part_fc[None],
        small_sums[6][None],
        part_proj[None],
        small_sums[7][None],
    )


STREAMS = 2
NRM, NMLP, UPS, BRN, ACT, GPRE, MIX, DQKV = range(8)
F32 = jnp.float32
LOW = jnp.bfloat16
MESH_ID = pl.DeviceIdType.MESH


def dot_nn(left, right):
    return lax.dot_general(left, right, (((1,), (0,)), ((), ())), preferred_element_type=F32)


def dot_nt(left, right):
    return lax.dot_general(left, right, (((1,), (1,)), ((), ())), preferred_element_type=F32)


def dot_tn(left, right):
    return lax.dot_general(left, right, (((0,), (0,)), ((), ())), preferred_element_type=F32)


def standard(rows):
    centred = rows - jnp.mean(rows, axis=-1, keepdims=True)
    scale = lax.rsqrt(jnp.mean(centred * centred, axis=-1, keepdims=True) + NORM_EPS)
    return centred * scale, scale


def standard_back(grad, xhat, scale):
    inner = jnp.mean(grad * xhat, axis=-1, keepdims=True)
    return scale * (grad - jnp.mean(grad, axis=-1, keepdims=True) - xhat * inner)


def column_sum(rows):
    return jnp.sum(rows.astype(F32), axis=0, keepdims=True)


def relay_kernel(names, *refs):
    r = types.SimpleNamespace(**dict(zip(names, refs)))
    a, c, t = (lax.axis_index(name) for name in ("section", "seq", "tensor"))
    lines = lax.axis_size("section")
    chips = lax.axis_size("tensor")
    rows, buckets, width = r.inputs.shape[1:]
    half_width = width // 2
    local = rows * chips
    total = 2 * local
    stream_rows = local // STREAMS
    head_width = r.wo_in.shape[0]
    heads = head_width // HDIM
    blocks = local // QB
    units = r.wp_in.shape[0]
    scale = HDIM ** (-0.5)
    streams = range(STREAMS)

    def remote(src, dst, send, recv, **target):
        return pltpu.make_async_remote_copy(
            src_ref=src,
            dst_ref=dst,
            send_sem=send,
            recv_sem=recv,
            device_id=target,
            device_id_type=MESH_ID,
        )

    def drain(ref, sem):
        pltpu.make_async_copy(ref, ref, sem).wait()

    def row_block(index, size):
        return pl.ds(pl.multiple_of(index * size, size), size)

    near_chip = t + 1 - 2 * (t % 2)
    over_chip = (t + 2) % 4
    across_chip = 3 - t
    middle_chip = (t == 1) | (t == 2)
    end_chip = (t == 0) | (t == 3)
    owned = stream_rows // 2
    mine = row_block(t - 1, owned)
    my_half = row_block(c, local)

    r.kv[...] = jnp.zeros(r.kv.shape, LOW)

    barrier = pltpu.get_barrier_semaphore()
    greeted = 0
    for line in range(lines):
        for chip in range(chips):
            for core in range(2):
                if (line, chip, core) != (0, 0, 0) and (core == 0 or line * chip == 0):
                    there = {
                        "section": (a + line) % lines,
                        "seq": (c + core) % 2,
                        "tensor": (t + chip) % chips,
                    }
                    pl.semaphore_signal(barrier, inc=1, device_id=there, device_id_type=MESH_ID)
                    greeted += 1
    pl.semaphore_wait(barrier, greeted)

    def beside(s):
        return s + 1 - 2 * (s % 2)

    def above(s):
        return (s + 2) % 4

    def store(p):
        return (r.wq, r.wo, r.wf, r.wp)[p]

    def source(p):
        return (r.wq_in, r.wo_in, r.wf_in, r.wp_in)[p]

    def height(p):
        return source(p).shape[0]

    def core_half(p, s, core):
        return store(p).at[s, row_block(core, height(p) // 2)]

    def first_hop(p, s, neighbour, which):
        return remote(
            source(p).at[row_block(c, height(p) // 2)],
            core_half(p, s, c),
            r.w_first_s.at[p, which],
            r.w_first_r.at[s, p],
            section=neighbour,
        )

    def second_hop(p, s, which):
        view = store(p).at[s, row_block(2 * c + which, height(p) // 4)]
        return remote(
            view, view, r.w_second_s.at[s, p], r.w_second_r.at[s, p, which], section=3 - s
        )

    def core_hop(p, s, core):
        view = core_half(p, s, core)
        return remote(view, view, r.w_core_s.at[s, p], r.w_core_r.at[s, p], seq=1 - c)

    def own_copy(p):
        return pltpu.make_async_copy(source(p), store(p).at[a], r.w_own.at[p])

    def pass_on(s, p, which):
        line = (beside(s), above(s))[which]

        @pl.when(a == line)
        def _():
            first_hop(p, s, line, which).wait_recv()
            second_hop(p, s, which).start()
            core_hop(p, s, c).start()

    def pass_all(s, pieces):
        for p in pieces:
            for which in range(2):
                pass_on(s, p, which)

    def pass_far(s, p):
        @pl.when(a == 3 - s)
        def _():
            second_hop(p, s, 0).wait_recv()
            second_hop(p, s, 1).wait_recv()
            core_hop(p, s, c).start()

    def need(s, p):
        @pl.when(s == 0)
        def _():
            if p < 2:
                pass_all(0, (p,))
            pass_far(0, p)

        @pl.when(a == s)
        def _():
            own_copy(p).wait()

        @pl.when(a != s)
        def _():
            core_hop(p, s, 1 - c).wait_recv()

    def small_copy(step, line, slot):
        return remote(
            r.small_own, r.small.at[slot], r.small_s.at[step], r.small_r.at[slot], section=line
        )

    def count_copy(step, line, slot):
        return remote(
            r.count_own.at[line],
            r.count.at[slot],
            r.count_s.at[step],
            r.count_r.at[slot],
            section=line,
        )

    singles = (r.ln1_gain, r.ln1_shift, r.ln2_gain, r.ln2_shift, r.b_out, r.b_proj)
    for place, single in enumerate(singles):
        r.small_own[place : place + 1] = single[...]
    r.small_own[6:7, :units] = r.b_fc[...]
    r.small_own[7:8, :head_width] = r.b_qv[0:1]
    r.small_own[7:8, half_width : half_width + head_width] = r.b_qv[1:2]
    for step in range(1, lines):
        small_copy(step - 1, (a + step) % lines, a).start()
    for p in range(4):
        for which, line in enumerate((beside(a), above(a))):
            first_hop(p, a, line, which).start()
    for p in range(4):
        own_copy(p).start()
    r.small[a] = r.small_own[...]

    def iota(shape, dimension):
        return lax.broadcasted_iota(jnp.int32, shape, dimension)

    square = jnp.where(iota((KSEL, KSEL), 0) == iota((KSEL, KSEL), 1), 1.0, 0.0).astype(LOW)
    position = iota((KSEL, total), 1).astype(F32)
    for pair in range(lines * heads):
        line, head = pair // heads, pair % heads
        columns = dot_nt(square, r.chosen[pair].astype(F32).astype(LOW))
        for block in range(blocks):
            pick = head * blocks + block
            r.count_own[line, pick : pick + 1, :] = jnp.sum(
                jnp.where(columns[:, block : block + 1] == position, 1.0, 0.0),
                axis=0,
                keepdims=True,
            )
    for step in range(1, lines):
        count_copy(step - 1, (a + step) % lines, a).start()
    r.count[a] = r.count_own[a]

    NEAR, OVER, ACROSS = range(3)

    def gather(buffer, s, kind, j, owner, target, slot):
        view = buffer.at[s, j, row_block(owner - 1, owned)]
        return remote(
            view, view, r.ag_s.at[kind, j, slot], r.ag_r.at[kind, j, slot], tensor=target
        )

    def used_before(s, kind):
        return s > 0 if kind < 2 else s < lines - 1

    def gather_start(buffer, s, kind, j):
        @pl.when(used_before(s, kind))
        def _():
            gather_sent(buffer, s, kind, j)

        gather(buffer, s, kind, j, t, over_chip, OVER).start()
        gather(buffer, s, kind, j, t, across_chip, ACROSS).start()
        gather(buffer, s, kind, j, t, near_chip, NEAR).start()

    def gather_wait(buffer, s, kind, j):
        @pl.when(middle_chip)
        def _():
            gather(buffer, s, kind, j, across_chip, across_chip, ACROSS).wait_recv()

        @pl.when(end_chip)
        def _():
            gather(buffer, s, kind, j, near_chip, near_chip, NEAR).wait_recv()
            gather(buffer, s, kind, j, over_chip, over_chip, OVER).wait_recv()

    def gather_sent(buffer, s, kind, j):
        gather(buffer, s, kind, j, t, over_chip, OVER).wait_send()
        gather(buffer, s, kind, j, t, across_chip, ACROSS).wait_send()
        gather(buffer, s, kind, j, t, near_chip, NEAR).wait_send()

    def scatter(s, kind, j, owner, slot):
        return remote(
            r.part.at[kind, j, row_block(owner - 1, owned)],
            r.arrived.at[s, kind, j, slot],
            r.rs_s.at[kind, j, slot],
            r.rs_r.at[kind, j, slot],
            tensor=owner,
        )

    def scatter_start(s, kind, j, product):
        @pl.when(used_before(s, kind))
        def _():
            scatter_sent(s, kind, j)

        r.part[kind, j] = product.astype(LOW)

        @pl.when(end_chip)
        def _():
            scatter(s, kind, j, over_chip, OVER).start()
            scatter(s, kind, j, near_chip, NEAR).start()

        @pl.when(middle_chip)
        def _():
            scatter(s, kind, j, across_chip, ACROSS).start()

    def scatter_sum(s, kind, j):
        result = r.part[kind, j, mine].astype(F32)
        for slot in (NEAR, ACROSS, OVER):
            scatter(s, kind, j, t, slot).wait_recv()
            result = result + r.arrived[s, kind, j, slot].astype(F32)
        return result

    def scatter_sent(s, kind, j):
        @pl.when(end_chip)
        def _():
            scatter(s, kind, j, over_chip, OVER).wait_send()
            scatter(s, kind, j, near_chip, NEAR).wait_send()

        @pl.when(middle_chip)
        def _():
            scatter(s, kind, j, across_chip, ACROSS).wait_send()

    own_rows = (r.nrm, r.nmlp, r.ups, r.brn, r.act, r.gpre, r.mix, r.dqkv)
    all_rows = (
        r.all_nrm,
        r.all_nmlp,
        r.all_ups,
        r.all_brn,
        r.all_act,
        r.all_gpre,
        r.all_mix,
        r.all_dqkv,
    )

    def rows_copy(index, s, same, stays=False):
        core = c if same else 1 - c
        src = own_rows[index].at[s]
        dst = all_rows[index].at[a, c]
        if index <= BRN:
            src = src.at[:, :, row_block(core, half_width)]
        recv = r.heads_r.at[a] if index == DQKV else r.rows_r.at[index]
        if stays:
            return pltpu.make_async_copy(src, dst, recv)
        if same:
            return remote(src, dst, r.rows_s.at[index, s, 0], recv, section=s)
        return remote(src, dst, r.rows_s.at[index, s, 1], recv, section=s, seq=1 - c)

    passed_rows = {UPS: r.pass_ups, GPRE: r.pass_gpre}
    places = {UPS: 0, GPRE: 1}

    def detour_copy(index):
        return remote(
            own_rows[index].at[0],
            passed_rows[index],
            r.pass_s.at[places[index]],
            r.pass_r.at[places[index]],
            section=1,
        )

    def passed_copies(index):
        copies = []
        for step in range(2 if index <= BRN else 1):
            core = (c + step) % 2
            src = passed_rows[index]
            if index <= BRN:
                src = src.at[:, :, row_block(core, half_width)]
            send = r.pass_on_s.at[places[index], step]
            dst = all_rows[index].at[3, c]
            copies.append(remote(src, dst, send, r.rows_r.at[index], section=0, seq=core))
        return copies

    def pass_rows(index):
        @pl.when(a == 1)
        def _():
            detour_copy(index).wait_recv()
            for copy in passed_copies(index):
                copy.start()

    def goes_direct(index, s):
        return jnp.logical_not((a == 3) & (s == 0)) if index in passed_rows else a >= 0

    def rows_start(index, s):
        if index in passed_rows:

            @pl.when((a == 3) & (s == 0))
            def _():
                detour_copy(index).start()

        @pl.when(a == s)
        def _():
            rows_copy(index, s, True, True).start()

        @pl.when((a != s) & goes_direct(index, s))
        def _():
            rows_copy(index, s, True).start()

        if index <= BRN:

            @pl.when(goes_direct(index, s))
            def _():
                rows_copy(index, s, False).start()

    def forward_rows(s):
        for index in (NRM, MIX, NMLP, ACT):
            rows_start(index, s)

    def rows_sent(index, s):
        @pl.when((a != s) & goes_direct(index, s))
        def _():
            rows_copy(index, s, True).wait_send()

        if index <= BRN:

            @pl.when(goes_direct(index, s))
            def _():
                rows_copy(index, s, False).wait_send()

    def share_copy(index, core):
        view = all_rows[index].at[:, core]
        return remote(view, view, r.share_s.at[index - ACT], r.share_r.at[index - ACT], seq=1 - c)

    def share_heads(line, core):
        view = r.all_dqkv.at[line, core]
        return remote(view, view, r.heads_s.at[line], r.heads_sr.at[line], seq=1 - c)

    def share(index):
        drain(all_rows[index].at[:, c], r.rows_r.at[index])
        share_copy(index, c).start()

    def norm_copy(s):
        return remote(
            r.norm_part.at[s], r.norm_all.at[a], r.norm_s.at[s], r.norm_r, section=s
        )

    def norm_start(s):
        @pl.when(a == s)
        def _():
            pltpu.make_async_copy(r.norm_part.at[s], r.norm_all.at[a], r.norm_r).start()

        @pl.when(a != s)
        def _():
            norm_copy(s).start()

    def home_copy(what, s, j):
        src, dst, send, recv = what
        chip = 2 * j + t - 1
        return remote(src.at[s, j], dst.at[a], send.at[s, j], recv, section=s, tensor=chip)

    def home_start(what, s):
        @pl.when(middle_chip)
        def _():
            for j in streams:
                home_copy(what, s, j).start()

    def home_sent(what, s):
        @pl.when(middle_chip)
        def _():
            for j in streams:
                home_copy(what, s, j).wait_send()

    out_home = (r.out_low, r.acts, r.out_s, r.out_r)
    grad_home = (r.grad_low, r.grads, r.grad_s, r.grad_r)

    length = r.lengths[a // buckets, a % buckets]
    key = iota((stream_rows, total), 1)
    for j in streams:
        query = c * local + j * stream_rows + iota((stream_rows, total), 0)
        r.near[j] = jnp.where((query >= key) & (query - key < WIN), 1.0, 0.0)
    key_row = iota((1, total), 1)

    def row_mask(place):
        return jnp.where(place < length, 1.0, 0.0)

    def stream_mask(j):
        return row_mask(c * local + j * stream_rows + iota((stream_rows, 1), 0))

    def multiplicity(s, j, head):
        block = j * stream_rows // QB
        pick = head * blocks + block
        limit = (c * blocks + block) * QB - WIN
        return r.near[j] + jnp.where(key_row <= limit, r.count[s, pick : pick + 1, :], 0.0)

    def head_cols(head):
        return slice(head * HDIM, (head + 1) * HDIM)

    def kv_copy(s, j):
        view = r.kv.at[s, :, j * stream_rows : (j + 1) * stream_rows]
        return remote(view, view, r.kv_s.at[s, j], r.kv_r.at[s, j], seq=1 - c)

    def dkv_copy(s):
        return remote(r.dkv_out.at[s], r.dkv_in.at[s], r.dkv_s.at[s], r.dkv_r.at[s], seq=1 - c)

    def own_sequence(ref):
        both = ref[a // buckets].astype(F32)
        picked = both[:, 0, :]
        for bucket in range(1, buckets):
            picked = jnp.where(a % buckets == bucket, both[:, bucket, :], picked)
        return picked

    def first_copy(stream):
        return remote(
            r.first_out, r.first_in.at[stream], r.first_s, r.first_r.at[stream], tensor=1 + t % 2
        )

    own_place = c * local + t * rows + iota((rows, 1), 0)
    r.first_out[0] = own_sequence(r.inputs).astype(LOW)
    r.first_out[1] = (own_sequence(r.cotangent) * row_mask(own_place)).astype(LOW)
    first_copy(t // 2).start()
    r.norm_part[...] = jnp.zeros_like(r.norm_part)

    def first_rows(j):
        @pl.when(middle_chip)
        def _():
            first_copy(j).wait_recv()
            r.hidden[j] = r.first_in[j, 0].astype(F32)
            r.upstream[j] = r.first_in[j, 1]

    def on_owner(stage):
        def run(s, j):
            @pl.when(middle_chip)
            def _():
                stage(s, j)

        return run

    @on_owner
    def enter(s, j):
        xhat, inverse = standard(r.hidden[j])
        r.xhat1[s, j] = xhat
        r.inv1[s, j] = jnp.broadcast_to(inverse, (owned, 128))
        r.nrm[s, j, mine] = (xhat * r.small[s, 0:1] + r.small[s, 1:2]).astype(LOW)
        gather_start(r.nrm, s, 0, j)

    def project(s, j):
        gather_wait(r.nrm, s, 0, j)
        normed = r.nrm[s, j]
        place = row_block(c * STREAMS + j, stream_rows)
        bias_v = r.small[s, 7:8, half_width : half_width + head_width]
        key_rows = dot_nt(normed, r.wq[s, head_width : 2 * head_width])
        value_rows = dot_nt(normed, r.wq[s, 2 * head_width : 3 * head_width]) + bias_v
        r.kv[s, 0, place] = key_rows.astype(LOW)
        r.kv[s, 1, place] = value_rows.astype(LOW)

    def ask(s, j):
        queries = dot_nt(r.nrm[s, j], r.wq[s, 0:head_width]) + r.small[s, 7:8, :head_width]
        r.qry[s, j] = queries.astype(LOW)

    def attend_line(s, j):
        mixed = []
        for head in range(heads):
            cols = head_cols(head)
            times = multiplicity(s, j, head)
            scores = scale * dot_nt(r.qry[s, j, :, cols], r.kv[s, 0, :, cols])
            scores = jnp.where(times > 0.0, scores, MASKED)
            top = jnp.max(scores, axis=-1, keepdims=True)
            terms = times * jnp.exp(scores - top)
            weights = terms / jnp.sum(terms, axis=-1, keepdims=True)
            r.soft[s, j, head] = weights
            mixed.append(dot_nn(weights.astype(LOW), r.kv[s, 1, :, cols]))
        r.mix[s, j] = (jnp.concatenate(mixed, axis=-1) * stream_mask(j)).astype(LOW)

    def leave_attention(s, j):
        scatter_start(s, 0, j, dot_nn(r.mix[s, j], r.wo[s]))

    @on_owner
    def between(s, j):
        middle = r.hidden[j] + scatter_sum(s, 0, j) + r.small[s, 4:5]
        r.middle[j] = middle
        xhat, inverse = standard(middle)
        r.xhat2[s, j] = xhat
        r.inv2[s, j] = jnp.broadcast_to(inverse, (owned, 128))
        r.nmlp[s, j, mine] = (xhat * r.small[s, 2:3] + r.small[s, 3:4]).astype(LOW)
        gather_start(r.nmlp, s, 1, j)

    def feed(s, j):
        gather_wait(r.nmlp, s, 1, j)
        before = dot_nn(r.nmlp[s, j], r.wf[s]) + r.small[s, 6:7, :units]
        bend = jnp.tanh(0.7978845608028654 * (before + 0.044715 * before * before * before))
        r.act[s, j] = (0.5 * before * (1.0 + bend)).astype(LOW)
        r.slope[s, j] = 0.5 * (1.0 + bend) + 0.5 * before * (1.0 - bend * bend) * (
            0.7978845608028654 * (1.0 + 3 * 0.044715 * before * before)
        )


    def leave_feed(s, j):
        scatter_start(s, 1, j, dot_nn(r.act[s, j], r.wp[s]))

    @on_owner
    def finish(s, j):
        result = r.middle[j] + scatter_sum(s, 1, j) + r.small[s, 5:6]
        r.out_low[s, j] = result.astype(LOW)
        r.hidden[j] = result.astype(LOW).astype(F32)

    def small_ready(s):
        @pl.when(a != s)
        def _():
            small_copy(0, a, s).wait_recv()

    small_ready(0)
    for j in streams:
        first_rows(j)
        enter(0, j)

    def forward(s, _):
        need(s, 0)
        need(s, 1)

        @pl.when(a != s)
        def _():
            count_copy(0, a, s).wait_recv()

        for j in streams:
            project(s, j)

            @pl.when(c == 0)
            def _():
                kv_copy(s, j).start()

            ask(s, j)
            if j == 0:

                @pl.when(c == 1)
                def _():
                    for other in streams:
                        kv_copy(s, other).wait_recv()

            attend_line(s, j)
            leave_attention(s, j)

        @pl.when(s == 0)
        def _():
            pass_all(0, (2,))
            for later in range(1, lines):
                pass_all(later, (0, 1, 2))

        @pl.when(s == 1)
        def _():
            pass_far(1, 2)
            pass_far(1, 3)
            for later in range(2, lines):
                for p in range(4):
                    pass_far(later, p)

        for j in streams:
            between(s, j)
        @pl.when(s == 0)
        def _():
            for later in range(lines):
                pass_all(later, (3,))

        need(s, 2)
        for j in streams:
            feed(s, j)
            if j == 0:
                need(s, 3)
            leave_feed(s, j)


        @pl.when(s >= 2)
        def _():
            forward_rows(s - 2)


        @pl.when(s + 1 < lines)
        def _():
            small_ready(s + 1)

        for j in streams:
            finish(s, j)

            @pl.when(s + 1 < lines)
            def _():
                enter(s + 1, j)

        home_start(out_home, s)

        @pl.when(s == 0)
        def _():
            pass_far(1, 0)
            pass_far(1, 1)

        return 0

    lax.fori_loop(0, lines, forward, 0)

    @on_owner
    def turn(s, j):
        upstream = r.upstream[j]
        r.ups[s, j, mine] = upstream
        gather_start(r.ups, s, 2, j)
        r.norm_part[s, 5:6] += column_sum(upstream)

    def feed_back(s, j):
        gather_wait(r.ups, s, 2, j)
        grad_pre = (dot_nt(r.ups[s, j], r.wp[s]) * r.slope[s, j]).astype(LOW)
        r.gpre[s, j] = grad_pre
        scatter_start(s, 2, j, dot_nt(grad_pre, r.wf[s]))
        r.norm_part[s, 6:7, :units] += column_sum(grad_pre)

    @on_owner
    def between_back(s, j):
        grad = scatter_sum(s, 2, j)
        xhat = r.xhat2[s, j]
        upstream = r.upstream[j].astype(F32)
        grad_middle = upstream + standard_back(
            grad * r.small[s, 2:3], xhat, r.inv2[s, j, :, 0:1]
        )
        r.middle[j] = grad_middle
        branch = grad_middle.astype(LOW)
        r.brn[s, j, mine] = branch
        gather_start(r.brn, s, 3, j)
        r.norm_part[s, 2:3] += column_sum(grad * xhat)
        r.norm_part[s, 3:4] += column_sum(grad)
        r.norm_part[s, 4:5] += column_sum(branch)

    def mixed_back(s, j):
        gather_wait(r.brn, s, 3, j)
        r.gmix[j] = (dot_nt(r.brn[s, j], r.wo[s]) * stream_mask(j)).astype(LOW)

    def attend_line_back(s, j):
        grad_q, grad_k, grad_v = [], [], []
        for head in range(heads):
            cols = head_cols(head)
            weights = r.soft[s, j, head]
            grad_head = r.gmix[j, :, cols]
            grad_weights = dot_nt(grad_head, r.kv[s, 1, :, cols])
            inner = jnp.sum(weights * grad_weights, axis=-1, keepdims=True)
            grad_scores = (weights * (grad_weights - inner)).astype(LOW)
            grad_k.append(scale * dot_tn(grad_scores, r.qry[s, j, :, cols]))
            grad_v.append(dot_tn(weights.astype(LOW), grad_head))
            grad_q.append(scale * dot_nn(grad_scores, r.kv[s, 0, :, cols]))
        for which, grad in enumerate((grad_k, grad_v)):
            grad = jnp.concatenate(grad, axis=-1)
            r.dkv_all[which] = grad if j == STREAMS - 1 else r.dkv_all[which] + grad
        grad_q = jnp.concatenate(grad_q, axis=-1).astype(LOW)
        r.dqkv[s, 0, j] = grad_q
        r.norm_part[s, 7:8, :head_width] += column_sum(grad_q)

    def join_keys(s, j):
        for which in range(2):
            joined = r.dkv_all[which, row_block(c * STREAMS + j, stream_rows)].astype(LOW)
            r.dqkv[s, 1 + which, j] = joined
            if which == 1:
                lanes = slice(half_width, half_width + head_width)
                r.norm_part[s, 7:8, lanes] += column_sum(joined)

    def leave_back(s, j):
        product = dot_nn(r.dqkv[s, 0, j], r.wq[s, 0:head_width])
        for which in range(1, 3):
            weight = r.wq[s, which * head_width : (which + 1) * head_width]
            product = product + dot_nn(r.dqkv[s, which, j], weight)
        scatter_start(s, 3, j, product)

    @on_owner
    def finish_back(s, j):
        grad = scatter_sum(s, 3, j)
        xhat = r.xhat1[s, j]
        result = r.middle[j] + standard_back(
            grad * r.small[s, 0:1], xhat, r.inv1[s, j, :, 0:1]
        )
        r.upstream[j] = result.astype(LOW)
        r.grad_low[s, j] = result.astype(LOW)
        r.norm_part[s, 0:1] += column_sum(grad * xhat)
        r.norm_part[s, 1:2] += column_sum(grad)

    last_first = tuple(reversed(streams))
    for j in last_first:
        turn(lines - 1, j)

    def backward(index, _):
        s = lines - 1 - index
        for j in last_first:
            feed_back(s, j)
        rows_start(UPS, s)
        rows_start(GPRE, s)

        @pl.when(index < 2)
        def _():
            forward_rows(lines - 2 + index)

        @pl.when(index == lines - 1)
        def _():
            share(ACT)
            share(MIX)

        for j in last_first:
            between_back(s, j)
        @pl.when(s == 0)
        def _():
            pass_rows(UPS)
            pass_rows(GPRE)

        for j in last_first:
            mixed_back(s, j)
            if j == 0:
                rows_start(BRN, s)
            attend_line_back(s, j)

            @pl.when(c == 1)
            def _():
                join_keys(s, j)
                leave_back(s, j)

        @pl.when(c == 1)
        def _():
            r.dkv_out[s] = r.dkv_all[:, 0:local].astype(LOW)
            dkv_copy(s).start()

        @pl.when(c == 0)
        def _():
            dkv_copy(s).wait_recv()
            r.dkv_all[:, 0:local] += r.dkv_in[s].astype(F32)
            for j in last_first:
                join_keys(s, j)
                leave_back(s, j)

        rows_start(DQKV, s)

        for j in last_first:
            finish_back(s, j)

            @pl.when(s > 0)
            def _():
                turn(s - 1, j)

        norm_start(s)
        home_start(grad_home, s)
        return 0

    lax.fori_loop(0, lines, backward, 0)

    share(GPRE)

    drain(r.norm_all, r.norm_r)
    slot = c * chips + t
    norm_sum = r.norm_all[0]
    for line in range(1, lines):
        norm_sum = norm_sum + r.norm_all[line]
    r.ends[slot] = norm_sum

    def ends_copy(step):
        core, chip = step // chips, step % chips
        view = r.ends.at[slot]
        return remote(
            view,
            view,
            r.ends_s.at[step - 1],
            r.ends_r,
            seq=(c + core) % 2,
            tensor=(t + chip) % chips,
        )

    for step in range(1, 2 * chips):
        ends_copy(step).start()

    for line in range(lines):
        drain(r.all_dqkv.at[line, c], r.heads_r.at[line])
        share_heads(line, c).start()

    for index in (UPS, GPRE):

        @pl.when(a == 3)
        def _():
            detour_copy(index).wait_send()

        @pl.when(a == 1)
        def _():
            for copy in passed_copies(index):
                copy.wait_send()

    for kind, buffer in enumerate((r.nrm, r.nmlp, r.ups, r.brn)):
        for j in streams:
            scatter_sent(0, kind, j)

            @pl.when(middle_chip)
            def _():
                gather_sent(buffer, 0, kind, j)

    for index in range(ACT):
        drain(all_rows[index], r.rows_r.at[index])
    for index in range(ACT, DQKV):
        share_copy(index, 1 - c).wait_recv()
        share_copy(index, c).wait_send()
    for line in range(lines):
        share_heads(line, 1 - c).wait_recv()
        share_heads(line, c).wait_send()
    drain(r.acts, r.out_r)
    drain(r.grads, r.grad_r)
    drain(r.ends.at[0 : 2 * chips - 1], r.ends_r)
    for step in range(1, 2 * chips):
        ends_copy(step).wait_send()
    for step in range(1, lines):
        small_copy(step - 1, (a + step) % lines, a).wait_send()
        count_copy(step - 1, (a + step) % lines, a).wait_send()
    for p in range(4):
        for which, line in enumerate((beside(a), above(a))):
            first_hop(p, a, line, which).wait_send()

    first_copy(t // 2).wait_send()

    def sent(s, _):
        home_sent(out_home, s)
        home_sent(grad_home, s)

        @pl.when(a != s)
        def _():
            norm_copy(s).wait_send()

        @pl.when(c == 0)
        def _():
            for j in streams:
                kv_copy(s, j).wait_send()

        @pl.when(c == 1)
        def _():
            dkv_copy(s).wait_send()

        for index in range(8):
            rows_sent(index, s)
        for p in range(4):

            @pl.when((a == beside(s)) | (a == above(s)))
            def _():
                second_hop(p, s, 0).wait_send()

            @pl.when(a != s)
            def _():
                core_hop(p, s, c).wait_send()

        return 0

    lax.fori_loop(0, lines, sent, 0)


def relay_call(inputs, cotangent, lengths, chosen, singles, weights):
    lines = lax.axis_size("section")
    chips = lax.axis_size("tensor")
    rows, buckets, width = inputs.shape[1:]
    local, total, half = rows * chips, 2 * rows * chips, width // 2
    head_width, units = weights["wo_in"].shape[0], weights["wp_in"].shape[0]
    heads = head_width // HDIM
    stream = local // STREAMS
    peers, owned = chips - 1, stream // 2
    vmem, dma = pltpu.VMEM, pltpu.SemaphoreType.DMA
    operands = dict(
        inputs=inputs,
        cotangent=cotangent,
        lengths=lengths,
        chosen=chosen,
        **singles,
        **weights,
    )

    def space(name):
        if name in weights:
            return pl.ANY
        return pltpu.SMEM if operands[name] is lengths else pltpu.VMEM

    sums = dict(
        acts=((lines, rows, width), LOW),
        grads=((lines, rows, width), LOW),
        ends=((2 * chips, 8, width), F32),
    )
    gathered = dict(
        all_nrm=((lines, 2, STREAMS, stream, half), LOW),
        all_nmlp=((lines, 2, STREAMS, stream, half), LOW),
        all_ups=((lines, 2, STREAMS, stream, half), LOW),
        all_brn=((lines, 2, STREAMS, stream, half), LOW),
        all_act=((lines, 2, STREAMS, stream, units), LOW),
        all_gpre=((lines, 2, STREAMS, stream, units), LOW),
        all_mix=((lines, 2, STREAMS, stream, head_width), LOW),
        all_dqkv=((lines, 2, 3, STREAMS, stream, head_width), LOW),
    )
    outputs = dict(**sums, **gathered)
    scratch = dict(
        wq=vmem((lines,) + weights["wq_in"].shape, LOW),
        wo=vmem((lines,) + weights["wo_in"].shape, LOW),
        wf=vmem((lines,) + weights["wf_in"].shape, LOW),
        wp=vmem((lines,) + weights["wp_in"].shape, LOW),
        small_own=vmem((8, width), F32),
        small=vmem((lines, 8, width), F32),
        count_own=vmem((lines, 8, total), F32),
        count=vmem((lines, 8, total), F32),
        hidden=vmem((STREAMS, owned, width), F32),
        middle=vmem((STREAMS, owned, width), F32),
        upstream=vmem((STREAMS, owned, width), LOW),
        first_out=vmem((2, owned, width), LOW),
        first_in=vmem((STREAMS, 2, owned, width), LOW),
        xhat1=vmem((lines, STREAMS, owned, width), F32),
        inv1=vmem((lines, STREAMS, owned, 128), F32),
        xhat2=vmem((lines, STREAMS, owned, width), F32),
        inv2=vmem((lines, STREAMS, owned, 128), F32),
        nrm=vmem((lines, STREAMS, stream, width), LOW),
        nmlp=vmem((lines, STREAMS, stream, width), LOW),
        ups=vmem((lines, STREAMS, stream, width), LOW),
        brn=vmem((lines, STREAMS, stream, width), LOW),
        act=vmem((lines, STREAMS, stream, units), LOW),
        gpre=vmem((lines, STREAMS, stream, units), LOW),
        slope=vmem((lines, STREAMS, stream, units), F32),
        mix=vmem((lines, STREAMS, stream, head_width), LOW),
        qry=vmem((lines, STREAMS, stream, head_width), LOW),
        gmix=vmem((STREAMS, stream, head_width), LOW),
        dqkv=vmem((lines, 3, STREAMS, stream, head_width), LOW),
        pass_ups=vmem((STREAMS, stream, width), LOW),
        pass_gpre=vmem((STREAMS, stream, units), LOW),
        kv=vmem((lines, 2, total, head_width), LOW),
        soft=vmem((lines, STREAMS, heads, stream, total), F32),
        near=vmem((STREAMS, stream, total), F32),
        dkv_all=vmem((2, total, head_width), F32),
        dkv_out=vmem((lines, 2, local, head_width), LOW),
        dkv_in=vmem((lines, 2, local, head_width), LOW),
        part=vmem((4, STREAMS, stream, width), LOW),
        arrived=vmem((lines, 4, STREAMS, peers, owned, width), LOW),
        out_low=vmem((lines, STREAMS, owned, width), LOW),
        grad_low=vmem((lines, STREAMS, owned, width), LOW),
        norm_part=vmem((lines, 8, width), F32),
        norm_all=vmem((lines, 8, width), F32),
        w_first_s=dma((4, 2)),
        w_first_r=dma((lines, 4)),
        w_second_s=dma((lines, 4)),
        w_second_r=dma((lines, 4, 2)),
        w_core_s=dma((lines, 4)),
        w_core_r=dma((lines, 4)),
        w_own=dma((4,)),
        small_s=dma((lines - 1,)),
        small_r=dma((lines,)),
        count_s=dma((lines - 1,)),
        count_r=dma((lines,)),
        ag_s=dma((4, STREAMS, peers)),
        ag_r=dma((4, STREAMS, peers)),
        rs_s=dma((4, STREAMS, peers)),
        rs_r=dma((4, STREAMS, peers)),
        kv_s=dma((lines, STREAMS)),
        kv_r=dma((lines, STREAMS)),
        dkv_s=dma((lines,)),
        dkv_r=dma((lines,)),
        rows_s=dma((8, lines, 2)),
        rows_r=dma((8,)),
        pass_s=dma((2,)),
        pass_r=dma((2,)),
        pass_on_s=dma((2, 2)),
        share_s=dma((4,)),
        share_r=dma((4,)),
        heads_r=dma((lines,)),
        heads_s=dma((lines,)),
        heads_sr=dma((lines,)),
        first_s=dma,
        first_r=dma((STREAMS,)),
        out_s=dma((lines, STREAMS)),
        out_r=dma,
        grad_s=dma((lines, STREAMS)),
        grad_r=dma,
        norm_s=dma((lines,)),
        norm_r=dma,
        ends_s=dma((2 * chips - 1,)),
        ends_r=dma,
    )
    names = tuple(operands) + tuple(outputs) + tuple(scratch)
    results = pl.pallas_call(
        functools.partial(relay_kernel, names),
        out_shape=[jax.ShapeDtypeStruct(shape, kind) for shape, kind in outputs.values()],
        in_specs=[pl.BlockSpec(memory_space=space(name)) for name in operands],
        out_specs=[
            pl.BlockSpec(memory_space=pl.ANY if name in gathered else pltpu.VMEM)
            for name in outputs
        ],
        scratch_shapes=list(scratch.values()),
        compiler_params=pltpu.CompilerParams(
            collective_id=0, has_side_effects=True, vmem_limit_bytes=60 * 2**20
        ),
        name="relay",
    )(*operands.values())
    return dict(zip(outputs, results))


def weights_kernel(names, *refs):
    r = types.SimpleNamespace(**dict(zip(names, refs)))
    micro_count, rows, buckets, width = r.activations.shape
    chips, units, head_width = r.ends.shape[0] // 2, r.all_act.shape[-1], r.all_mix.shape[-1]
    lines = r.acts.shape[0]
    loads = [
        pltpu.make_async_copy(source, target, r.load_sem.at[place])
        for place, (source, target) in enumerate(
            (
                (r.all_act, r.act),
                (r.all_ups, r.ups),
                (r.all_nmlp, r.nmlp),
                (r.all_gpre, r.gpre),
                (r.all_mix, r.mix),
                (r.all_brn, r.brn),
                (r.all_nrm, r.nrm),
                (r.all_dqkv, r.dqkv),
            )
        )
    ]
    stores = [
        pltpu.make_async_copy(source, target, r.store_sem.at[place])
        for place, (source, target) in enumerate(
            (
                (r.own_proj, r.w_proj),
                (r.own_fc, r.w_fc),
                (r.own_out, r.w_out),
                (r.own_qkv, r.w_qkv),
            )
        )
    ]
    for load in loads:
        load.start()

    sums = r.ends[0]
    for other in range(1, 2 * chips):
        sums = sums + r.ends[other]
    singles = (r.ln1_gain, r.ln1_shift, r.ln2_gain, r.ln2_shift, r.b_out, r.b_proj)
    for place, single in enumerate(singles):
        single[...] = sums[place : place + 1]
    for chip in range(chips):
        both = r.ends[chip] + r.ends[chips + chip]
        r.b_fc[:, chip * units : (chip + 1) * units] = both[6:7, :units]
        here = slice(chip * head_width, (chip + 1) * head_width)
        r.b_qv[0:1, here] = both[7:8, :head_width]
        r.b_qv[1:2, here] = both[7:8, width // 2 : width // 2 + head_width]
    for target, source in ((r.activations, r.acts), (r.in_grads, r.grads)):
        for micro in range(micro_count):
            rows_of = [
                source[micro * buckets + bucket].astype(F32)[:, None, :]
                for bucket in range(buckets)
            ]
            target[micro] = jnp.concatenate(rows_of, axis=1).astype(LOW)

    def flat(array):
        return array.reshape(lines * 2 * chips * rows, array.shape[-1])

    loads[0].wait()
    loads[1].wait()
    r.own_proj[...] = dot_tn(flat(r.act[...]), flat(r.ups[...]))
    stores[0].start()
    loads[2].wait()
    loads[3].wait()
    r.own_fc[...] = dot_tn(flat(r.nmlp[...]), flat(r.gpre[...]))
    stores[1].start()
    loads[4].wait()
    loads[5].wait()
    r.own_out[...] = dot_tn(flat(r.mix[...]), flat(r.brn[...]))
    stores[2].start()
    loads[6].wait()
    loads[7].wait()
    nrm = flat(r.nrm[...])
    for which in range(3):
        r.own_qkv[which] = dot_tn(flat(r.dqkv[:, :, which]), nrm)
    stores[3].start()
    for store in stores:
        store.wait()


def weights_call(relayed, inputs_shape, head_width, units):
    chips = lax.axis_size("tensor")
    width = inputs_shape[-1]
    half = width // 2
    outputs = dict(
        activations=(inputs_shape, LOW),
        in_grads=(inputs_shape, LOW),
        ln1_gain=((1, width), F32),
        ln1_shift=((1, width), F32),
        w_qkv=((3, head_width, half), F32),
        b_qv=((2, width), F32),
        w_out=((head_width, half), F32),
        b_out=((1, width), F32),
        ln2_gain=((1, width), F32),
        ln2_shift=((1, width), F32),
        w_fc=((half, units), F32),
        b_fc=((1, chips * units), F32),
        w_proj=((units, half), F32),
        b_proj=((1, width), F32),
    )
    rows = ("act", "ups", "nmlp", "gpre", "mix", "brn", "nrm", "dqkv")
    own = dict(own_proj="w_proj", own_fc="w_fc", own_out="w_out", own_qkv="w_qkv")
    scratch = {name: pltpu.VMEM(relayed["all_" + name].shape, LOW) for name in rows}
    scratch.update({name: pltpu.VMEM(outputs[of][0], F32) for name, of in own.items()})
    scratch["load_sem"] = pltpu.SemaphoreType.DMA((8,))
    scratch["store_sem"] = pltpu.SemaphoreType.DMA((4,))
    whole, apart = pl.BlockSpec(memory_space=pltpu.VMEM), pl.BlockSpec(memory_space=pl.ANY)
    small = ("acts", "grads", "ends")
    return pl.pallas_call(
        functools.partial(weights_kernel, tuple(relayed) + tuple(outputs) + tuple(scratch)),
        out_shape=[jax.ShapeDtypeStruct(shape, kind) for shape, kind in outputs.values()],
        in_specs=[whole if name in small else apart for name in relayed],
        out_specs=[apart if name in own.values() else whole for name in outputs],
        scratch_shapes=list(scratch.values()),
        compiler_params=pltpu.CompilerParams(vmem_limit_bytes=60 * 2**20),
        name="weight_gradients",
    )(*relayed.values())


def on_line(
    inputs,
    cotangent,
    lengths,
    chosen,
    ln1_gain,
    ln1_shift,
    w_qkv,
    b_qv,
    w_out,
    b_out,
    ln2_gain,
    ln2_shift,
    w_fc,
    b_fc,
    w_proj,
    b_proj,
):
    head_width, units = w_out.shape[1], w_fc.shape[2]
    singles = dict(
        ln1_gain=ln1_gain,
        ln1_shift=ln1_shift,
        ln2_gain=ln2_gain,
        ln2_shift=ln2_shift,
        b_out=b_out,
        b_proj=b_proj,
        b_fc=b_fc,
        b_qv=b_qv[0],
    )
    weights = dict(
        wq_in=jnp.swapaxes(w_qkv[0], 1, 2).reshape(-1, inputs.shape[-1]),
        wo_in=w_out[0],
        wf_in=w_fc[0],
        wp_in=w_proj[0],
    )
    picks = chosen.reshape((-1,) + chosen.shape[-2:])
    relayed = relay_call(inputs, cotangent, lengths, picks, singles, weights)
    results = list(weights_call(relayed, inputs.shape, head_width, units))
    results[4] = jnp.swapaxes(results[4], 1, 2)
    vectors = (2, 3, 7, 8, 9, 11, 13)
    return tuple(
        result if place in vectors else result[None] for place, result in enumerate(results)
    )


def fits_lines(mesh):
    return mesh.shape["section"] == 4 and mesh.shape["seq"] == 2 and mesh.shape["tensor"] == 4


def solution(mesh):
    placed = (
        P(None, ("seq", "tensor"), None, None),
        P(None, ("seq", "tensor"), None, None),
        P(),
        P("section", None, None, "tensor", "seq", None),
        P("section", None),
        P("section", None),
        P("section", None, None, "tensor"),
        P("section", None, "tensor"),
        P("section", "tensor", None),
        P("section", None),
        P("section", None),
        P("section", None),
        P("section", None, "tensor"),
        P("section", "tensor"),
        P("section", "tensor", None),
        P("section", None),
    )
    return jax.shard_map(
        on_line if fits_lines(mesh) else on_device,
        mesh=mesh,
        in_specs=placed,
        out_specs=(
            P("section", None, ("seq", "tensor"), None, None),
            P("section", None, ("seq", "tensor"), None, None),
            P("section", None),
            P("section", None),
            P("section", None, "seq", "tensor"),
            P("section", None, None),
            P("section", "tensor", "seq"),
            P("section", None),
            P("section", None),
            P("section", None),
            P("section", "seq", "tensor"),
            P("section", None),
            P("section", "tensor", "seq"),
            P("section", None),
        ),
        check_vma=False,
    )
```

```python
import functools
import types

import jax
import jax.numpy as jnp
from jax import lax
from jax.experimental import pallas as pl
from jax.experimental.pallas import tpu as pltpu
from jax.sharding import PartitionSpec as P

HDIM = 64
WIN = 64
QB = 64
KSEL = 64


NORM_EPS = 1e-05
MASKED = -1000000000.0


def from_behind(value, axis, steps):
    count = lax.axis_size(axis)
    first, last = (max(0, -steps), min(count, count - steps))
    return lax.ppermute(value, axis, [(source, source + steps) for source in range(first, last)])


def layer_norm(values, gain, shift):
    average = jnp.mean(values, axis=-1, keepdims=True)
    centred = values - average
    variance = jnp.mean(centred * centred, axis=-1, keepdims=True)
    return centred * lax.rsqrt(variance + NORM_EPS) * gain + shift


def gelu_tanh(values):
    return (
        0.5
        * values
        * (1.0 + jnp.tanh(0.7978845608028654 * (values + 0.044715 * values * values * values)))
    )


def gather_rows(row_block):
    return lax.all_gather(row_block, "tensor", axis=0, tiled=True)


def scatter_product(left_rows, weight, formula):
    return lax.psum_scatter(
        jnp.einsum(formula, left_rows, weight, preferred_element_type=jnp.float32).astype(
            jnp.bfloat16
        ),
        "tensor",
        scatter_dimension=0,
        tiled=True,
    ).astype(jnp.float32)


def near_slabs(full_rows, seq_start, seq_first, length_local):
    buckets = full_rows.shape[1]
    heads_local = full_rows.shape[2] // HDIM
    blocks = length_local // QB
    earlier = lax.dynamic_slice_in_dim(full_rows, jnp.maximum(seq_start - WIN, 0), WIN, 0)
    earlier = jnp.where(seq_first, jnp.zeros_like(earlier), earlier)
    local_part = lax.dynamic_slice_in_dim(full_rows, seq_start, length_local, 0)
    segment = jnp.concatenate([earlier, local_part], 0).reshape(
        length_local + WIN, buckets, heads_local, HDIM
    )
    return jnp.concatenate(
        [
            segment[offset_index * QB : offset_index * QB + length_local].reshape(
                blocks, QB, buckets, heads_local, HDIM
            )
            for offset_index in range(WIN // QB + 1)
        ],
        1,
    )


def far_rows(full_rows, flat_index):
    total_rows, buckets, feature_width = full_rows.shape
    heads_local = feature_width // HDIM
    return jnp.take(full_rows.reshape(total_rows * buckets * heads_local, HDIM), flat_index, axis=0)


def key_geometry(chosen_now, seq_start, blocks):
    buckets, heads_local = (chosen_now.shape[0], chosen_now.shape[1])
    bucket_ids = lax.broadcasted_iota(jnp.int32, chosen_now.shape, 0)
    head_ids = lax.broadcasted_iota(jnp.int32, chosen_now.shape, 1)
    flat_index = (chosen_now * buckets + bucket_ids) * heads_local + head_ids
    block_start = seq_start + QB * lax.broadcasted_iota(jnp.int32, (blocks, 1, 1), 0)
    query_ids = lax.broadcasted_iota(jnp.int32, (1, QB, 1), 1)
    key_ids = lax.broadcasted_iota(jnp.int32, (1, 1, WIN + QB), 2)
    distance = query_ids + WIN - key_ids
    near_ok = (distance >= 0) & (distance < WIN) & (block_start + key_ids - WIN >= 0)
    far_ok = chosen_now + WIN <= block_start.reshape(1, 1, blocks, 1)
    near_mask = jnp.broadcast_to(
        near_ok[:, None, None], (blocks, buckets, heads_local, QB, WIN + QB)
    )
    far_mask = jnp.broadcast_to(
        jnp.transpose(far_ok, (2, 0, 1, 3))[:, :, :, None, :],
        (blocks, buckets, heads_local, QB, KSEL),
    )
    return (flat_index, jnp.concatenate([near_mask, far_mask], -1))


def attention_setup(queries, key_rows, value_rows, chosen_now, seq_start, seq_first):
    length_local, buckets, feature_width = queries.shape
    heads_local = feature_width // HDIM
    blocks = length_local // QB
    query_blocks = queries.reshape(blocks, QB, buckets, heads_local, HDIM)
    flat_index, key_mask = key_geometry(chosen_now, seq_start, blocks)
    near_keys = near_slabs(key_rows, seq_start, seq_first, length_local)
    near_values = near_slabs(value_rows, seq_start, seq_first, length_local)
    far_keys = far_rows(key_rows, flat_index)
    far_values = far_rows(value_rows, flat_index)
    near_scores = jnp.einsum(
        "bqnhe,btnhe->bnhqt", query_blocks, near_keys, preferred_element_type=jnp.float32
    )
    far_scores = jnp.einsum(
        "bqnhe,nhbke->bnhqk", query_blocks, far_keys, preferred_element_type=jnp.float32
    )
    scores = jnp.where(
        key_mask, HDIM ** (-0.5) * jnp.concatenate([near_scores, far_scores], -1), MASKED
    )
    return (query_blocks, near_keys, near_values, far_keys, far_values, flat_index, scores)


def attend(queries, key_rows, value_rows, chosen_now, seq_start, seq_first):
    query_blocks, near_keys, near_values, far_keys, far_values, flat_index, scores = (
        attention_setup(queries, key_rows, value_rows, chosen_now, seq_start, seq_first)
    )
    span = WIN + QB
    row_top = jnp.max(scores, -1, keepdims=True)
    exp_terms = jnp.exp(scores - row_top)
    row_total = jnp.sum(exp_terms, -1, keepdims=True)
    softmax_low = (exp_terms / row_total).astype(jnp.bfloat16)
    near_part = jnp.einsum(
        "bnhqt,btnhe->bqnhe",
        softmax_low[..., :span],
        near_values,
        preferred_element_type=jnp.float32,
    )
    far_part = jnp.einsum(
        "bnhqk,nhbke->bqnhe",
        softmax_low[..., span:],
        far_values,
        preferred_element_type=jnp.float32,
    )
    return ((near_part + far_part).reshape(queries.shape), row_top + jnp.log(row_total))


def spread_back(near_grad, far_grad, flat_index, seq_start, seq_first, total_rows):
    blocks, span, buckets, heads_local, head_size = near_grad.shape
    length_local = blocks * QB
    feature_width = heads_local * head_size
    segment = jnp.zeros((length_local + WIN, buckets, heads_local, head_size), jnp.float32)
    for offset_index in range(WIN // QB + 1):
        piece = near_grad[:, offset_index * QB : (offset_index + 1) * QB].reshape(
            length_local, buckets, heads_local, head_size
        )
        segment = segment.at[offset_index * QB : offset_index * QB + length_local].add(piece)
    full_rows = jnp.zeros((total_rows * buckets * heads_local, head_size), jnp.float32)
    full_rows = full_rows.at[flat_index.reshape(-1)].add(far_grad.reshape(-1, head_size))
    full_rows = full_rows.reshape(total_rows, buckets, feature_width)
    local_part = segment[WIN:].reshape(length_local, buckets, feature_width)
    earlier = jnp.where(seq_first, 0.0, segment[:WIN].reshape(WIN, buckets, feature_width))
    full_rows = lax.dynamic_update_slice_in_dim(
        full_rows,
        lax.dynamic_slice_in_dim(full_rows, seq_start, length_local, 0) + local_part,
        seq_start,
        0,
    )
    earlier_start = jnp.maximum(seq_start - WIN, 0)
    full_rows = lax.dynamic_update_slice_in_dim(
        full_rows,
        lax.dynamic_slice_in_dim(full_rows, earlier_start, WIN, 0) + earlier,
        earlier_start,
        0,
    )
    return full_rows


def attend_back(
    queries, key_rows, value_rows, chosen_now, seq_start, seq_first, log_total, grad_mixed
):
    query_blocks, near_keys, near_values, far_keys, far_values, flat_index, scores = (
        attention_setup(queries, key_rows, value_rows, chosen_now, seq_start, seq_first)
    )
    span = WIN + QB
    score_scale = HDIM ** (-0.5)
    grad_blocks = grad_mixed.reshape(query_blocks.shape)
    weights_full = jnp.exp(scores - log_total)
    softmax_low = weights_full.astype(jnp.bfloat16)
    grad_near_weights = jnp.einsum(
        "bqnhe,btnhe->bnhqt", grad_blocks, near_values, preferred_element_type=jnp.float32
    )
    grad_far_weights = jnp.einsum(
        "bqnhe,nhbke->bnhqk", grad_blocks, far_values, preferred_element_type=jnp.float32
    )
    grad_weights = jnp.concatenate([grad_near_weights, grad_far_weights], -1)
    row_dot = jnp.sum(weights_full * grad_weights, -1, keepdims=True)
    grad_scores = (weights_full * (grad_weights - row_dot)).astype(jnp.bfloat16)
    grad_near, grad_far = (grad_scores[..., :span], grad_scores[..., span:])
    grad_queries = score_scale * (
        jnp.einsum("bnhqt,btnhe->bqnhe", grad_near, near_keys, preferred_element_type=jnp.float32)
        + jnp.einsum("bnhqk,nhbke->bqnhe", grad_far, far_keys, preferred_element_type=jnp.float32)
    )
    near_key_grad = score_scale * jnp.einsum(
        "bnhqt,bqnhe->btnhe", grad_near, query_blocks, preferred_element_type=jnp.float32
    )
    far_key_grad = score_scale * jnp.einsum(
        "bnhqk,bqnhe->nhbke", grad_far, query_blocks, preferred_element_type=jnp.float32
    )
    near_value_grad = jnp.einsum(
        "bnhqt,bqnhe->btnhe",
        softmax_low[..., :span],
        grad_blocks,
        preferred_element_type=jnp.float32,
    )
    far_value_grad = jnp.einsum(
        "bnhqk,bqnhe->nhbke",
        softmax_low[..., span:],
        grad_blocks,
        preferred_element_type=jnp.float32,
    )
    total_rows = key_rows.shape[0]
    key_grad = spread_back(
        near_key_grad, far_key_grad, flat_index, seq_start, seq_first, total_rows
    )
    value_grad = spread_back(
        near_value_grad, far_value_grad, flat_index, seq_start, seq_first, total_rows
    )
    return (grad_queries.reshape(queries.shape), key_grad, value_grad)


def forward_pass(hidden, params, chosen_now, query_mask, seq_start, seq_first, finish):
    (
        ln1_gain,
        ln1_shift,
        w_qkv,
        b_qv,
        w_out,
        b_out,
        ln2_gain,
        ln2_shift,
        w_fc,
        b_fc,
        w_proj,
        b_proj,
    ) = params
    hidden_wide = hidden.astype(jnp.float32)
    normed_all = gather_rows(layer_norm(hidden_wide, ln1_gain, ln1_shift).astype(jnp.bfloat16))
    projected = jnp.einsum("pnd,jdc->jpnc", normed_all, w_qkv, preferred_element_type=jnp.float32)
    queries = (projected[0] + b_qv[0]).astype(jnp.bfloat16)
    key_rows, value_rows = (
        lax.all_gather(projected[1].astype(jnp.bfloat16), "seq", axis=0, tiled=True),
        lax.all_gather((projected[2] + b_qv[1]).astype(jnp.bfloat16), "seq", axis=0, tiled=True),
    )
    attended, log_total = attend(queries, key_rows, value_rows, chosen_now, seq_start, seq_first)
    mixed_rows = (attended * query_mask[:, :, None]).astype(jnp.bfloat16)
    middle = hidden_wide + scatter_product(mixed_rows, w_out, "pnc,cd->pnd") + b_out
    normed_mlp = gather_rows(layer_norm(middle, ln2_gain, ln2_shift).astype(jnp.bfloat16))
    pre_active = (
        jnp.einsum("pnd,df->pnf", normed_mlp, w_fc, preferred_element_type=jnp.float32) + b_fc
    )
    active = gelu_tanh(pre_active).astype(jnp.bfloat16)
    if not finish:
        return (
            normed_all,
            queries,
            key_rows,
            value_rows,
            log_total,
            mixed_rows,
            middle,
            normed_mlp,
            pre_active,
            active,
        )
    output = (middle + scatter_product(active, w_proj, "pnf,fd->pnd") + b_proj).astype(jnp.bfloat16)
    return (output, (key_rows, value_rows))


def backward_pass(hidden, upstream, params, chosen_now, query_mask, seq_start, seq_first):
    (
        ln1_gain,
        ln1_shift,
        w_qkv,
        b_qv,
        w_out,
        b_out,
        ln2_gain,
        ln2_shift,
        w_fc,
        b_fc,
        w_proj,
        b_proj,
    ) = params
    (
        normed_all,
        queries,
        key_rows,
        value_rows,
        log_total,
        mixed_rows,
        middle,
        normed_mlp,
        pre_active,
        active,
    ) = forward_pass(hidden, params, chosen_now, query_mask, seq_start, seq_first, False)
    upstream_all = gather_rows(upstream)
    grad_w_proj = jnp.einsum(
        "pnf,pnd->fd", active, upstream_all, preferred_element_type=jnp.float32
    )
    grad_b_proj = jnp.sum(upstream.astype(jnp.float32), axis=(0, 1))
    grad_active = jnp.einsum(
        "pnd,fd->pnf", upstream_all, w_proj, preferred_element_type=jnp.float32
    )
    unused_value, gelu_pull = jax.vjp(gelu_tanh, pre_active)
    grad_pre = gelu_pull(grad_active)[0].astype(jnp.bfloat16)
    grad_w_fc = jnp.einsum("pnd,pnf->df", normed_mlp, grad_pre, preferred_element_type=jnp.float32)
    grad_b_fc = jnp.sum(grad_pre.astype(jnp.float32), axis=(0, 1))
    grad_normed_mlp = scatter_product(grad_pre, w_fc, "pnf,df->pnd")
    unused_norm, second_pull = jax.vjp(layer_norm, middle, ln2_gain, ln2_shift)
    grad_mid_norm, grad_ln2_gain, grad_ln2_shift = second_pull(grad_normed_mlp)
    grad_middle = upstream.astype(jnp.float32) + grad_mid_norm
    grad_branch = grad_middle.astype(jnp.bfloat16)
    grad_b_out = jnp.sum(grad_branch.astype(jnp.float32), axis=(0, 1))
    branch_all = gather_rows(grad_branch)
    grad_w_out = jnp.einsum(
        "pnc,pnd->cd", mixed_rows, branch_all, preferred_element_type=jnp.float32
    )
    grad_mixed = jnp.einsum(
        "pnd,cd->pnc", branch_all, w_out, preferred_element_type=jnp.float32
    ).astype(jnp.bfloat16) * query_mask[:, :, None].astype(jnp.bfloat16)
    grad_queries, key_grad_all, value_grad_all = attend_back(
        queries, key_rows, value_rows, chosen_now, seq_start, seq_first, log_total, grad_mixed
    )
    key_grad, value_grad = (
        lax.psum_scatter(
            key_grad_all.astype(jnp.bfloat16), "seq", scatter_dimension=0, tiled=True
        ).astype(jnp.float32),
        lax.psum_scatter(
            value_grad_all.astype(jnp.bfloat16), "seq", scatter_dimension=0, tiled=True
        ).astype(jnp.float32),
    )
    grad_project = jnp.stack(
        [
            grad_queries.astype(jnp.bfloat16),
            key_grad.astype(jnp.bfloat16),
            value_grad.astype(jnp.bfloat16),
        ],
        2,
    )
    grad_w_qkv = jnp.einsum(
        "pnd,pnjc->jdc", normed_all, grad_project, preferred_element_type=jnp.float32
    )
    grad_b_qv = jnp.sum(grad_project[:, :, 0::2].astype(jnp.float32), axis=(0, 1))
    grad_normed = scatter_product(grad_project, w_qkv, "pnjc,jdc->pnd")
    unused_first, first_pull = jax.vjp(layer_norm, hidden.astype(jnp.float32), ln1_gain, ln1_shift)
    grad_in_norm, grad_ln1_gain, grad_ln1_shift = first_pull(grad_normed)
    grad_hidden = (grad_middle + grad_in_norm).astype(jnp.bfloat16)
    block_grads = (
        grad_ln1_gain,
        grad_ln1_shift,
        grad_w_qkv,
        grad_b_qv,
        grad_w_out,
        grad_b_out,
        grad_ln2_gain,
        grad_ln2_shift,
        grad_w_fc,
        grad_b_fc,
        grad_w_proj,
        grad_b_proj,
    )
    return (grad_hidden, block_grads)


def on_device(
    inputs,
    cotangent,
    lengths,
    chosen,
    ln1_gain,
    ln1_shift,
    w_qkv,
    b_qv,
    w_out,
    b_out,
    ln2_gain,
    ln2_shift,
    w_fc,
    b_fc,
    w_proj,
    b_proj,
):
    params = tuple(
        (
            weight_array[0]
            for weight_array in (
                ln1_gain,
                ln1_shift,
                w_qkv,
                b_qv,
                w_out,
                b_out,
                ln2_gain,
                ln2_shift,
                w_fc,
                b_fc,
                w_proj,
                b_proj,
            )
        )
    )
    section_index = lax.axis_index("section")
    section_count = lax.axis_size("section")
    seq_index = lax.axis_index("seq")
    tensor_index = lax.axis_index("tensor")
    tensor_count = lax.axis_size("tensor")
    micro_count, rows_local, buckets, feature_width = inputs.shape
    length_local = rows_local * tensor_count
    heads_width = w_qkv.shape[-1]
    seq_start = seq_index * length_local
    seq_first = seq_index == 0
    positions = seq_start + lax.broadcasted_iota(jnp.int32, (micro_count, length_local, buckets), 1)
    mask_all = (positions < lengths[:, None, :]).astype(jnp.float32)
    mask_rows = lax.dynamic_slice_in_dim(mask_all, tensor_index * rows_local, rows_local, 1)
    step_count = micro_count + section_count - 1
    chosen_section = chosen[0]
    received = jnp.zeros((rows_local, buckets, feature_width), jnp.bfloat16)
    stored = jnp.zeros((micro_count, rows_local, buckets, feature_width), jnp.bfloat16)
    outputs = jnp.zeros_like(stored)
    for step_index in range(step_count):
        micro_index = step_index - section_index
        running = (micro_index >= 0) & (micro_index < micro_count)
        slot_index = jnp.clip(micro_index, 0, micro_count - 1)
        block_in = jnp.where(
            section_index == 0, lax.dynamic_index_in_dim(inputs, slot_index, 0, False), received
        )
        chosen_now = lax.dynamic_index_in_dim(chosen_section, slot_index, 0, False)
        query_mask = lax.dynamic_index_in_dim(mask_all, slot_index, 0, False)
        result, key_pair = forward_pass(
            block_in, params, chosen_now, query_mask, seq_start, seq_first, True
        )
        stored = jnp.where(
            running, lax.dynamic_update_index_in_dim(stored, block_in, slot_index, 0), stored
        )
        outputs = jnp.where(
            running, lax.dynamic_update_index_in_dim(outputs, result, slot_index, 0), outputs
        )
        received = from_behind(result, "section", 1)
    back_received = jnp.zeros((rows_local, buckets, feature_width), jnp.bfloat16)
    in_grads = jnp.zeros_like(stored)
    totals = None
    for step_index in range(step_count):
        micro_index = step_index - (section_count - 1 - section_index)
        running = (micro_index >= 0) & (micro_index < micro_count)
        slot_index = jnp.clip(micro_index, 0, micro_count - 1)
        chosen_now = lax.dynamic_index_in_dim(chosen_section, slot_index, 0, False)
        query_mask = lax.dynamic_index_in_dim(mask_all, slot_index, 0, False)
        local_mask = lax.dynamic_index_in_dim(mask_rows, slot_index, 0, False)
        top_grad = (
            lax.dynamic_index_in_dim(cotangent, slot_index, 0, False).astype(jnp.float32)
            * local_mask[:, :, None]
        ).astype(jnp.bfloat16)
        upstream = jnp.where(section_index == section_count - 1, top_grad, back_received)
        hidden = lax.dynamic_index_in_dim(stored, slot_index, 0, False)
        grad_hidden, block_grads = backward_pass(
            hidden, upstream, params, chosen_now, query_mask, seq_start, seq_first
        )
        block_grads = tuple(
            (jnp.where(running, grad_part, jnp.zeros_like(grad_part)) for grad_part in block_grads)
        )
        totals = (
            block_grads
            if step_index == 0
            else tuple(
                (total_part + grad_part for total_part, grad_part in zip(totals, block_grads))
            )
        )
        in_grads = jnp.where(
            running, lax.dynamic_update_index_in_dim(in_grads, grad_hidden, slot_index, 0), in_grads
        )
        back_received = from_behind(grad_hidden, "section", -1)
    (
        sum_ln1_gain,
        sum_ln1_shift,
        sum_w_qkv,
        sum_b_qv,
        sum_w_out,
        sum_b_out,
        sum_ln2_gain,
        sum_ln2_shift,
        sum_w_fc,
        sum_b_fc,
        sum_w_proj,
        sum_b_proj,
    ) = totals
    part_qkv, part_out, part_fc, part_proj = (
        lax.psum_scatter(
            sum_w_qkv.astype(jnp.bfloat16), "seq", scatter_dimension=1, tiled=True
        ).astype(jnp.float32),
        lax.psum_scatter(
            sum_w_out.astype(jnp.bfloat16), "seq", scatter_dimension=1, tiled=True
        ).astype(jnp.float32),
        lax.psum_scatter(
            sum_w_fc.astype(jnp.bfloat16), "seq", scatter_dimension=0, tiled=True
        ).astype(jnp.float32),
        lax.psum_scatter(
            sum_w_proj.astype(jnp.bfloat16), "seq", scatter_dimension=1, tiled=True
        ).astype(jnp.float32),
    )
    bias_qv = lax.dynamic_update_slice_in_dim(
        jnp.zeros((2, feature_width), jnp.float32), sum_b_qv, tensor_index * heads_width, 1
    )
    units_local = sum_b_fc.shape[0]
    bias_fc = lax.dynamic_update_slice_in_dim(
        jnp.zeros((units_local * tensor_count,), jnp.float32),
        sum_b_fc,
        tensor_index * units_local,
        0,
    )
    small_sums = lax.psum(
        (
            sum_ln1_gain,
            sum_ln1_shift,
            bias_qv,
            sum_b_out,
            sum_ln2_gain,
            sum_ln2_shift,
            bias_fc,
            sum_b_proj,
        ),
        ("seq", "tensor"),
    )
    return (
        outputs[None],
        in_grads[None],
        small_sums[0][None],
        small_sums[1][None],
        part_qkv[None],
        small_sums[2][None],
        part_out[None],
        small_sums[3][None],
        small_sums[4][None],
        small_sums[5][None],
        part_fc[None],
        small_sums[6][None],
        part_proj[None],
        small_sums[7][None],
    )


STREAMS = 2
NRM, NMLP, UPS, BRN, ACT, GPRE, MIX, DQKV = range(8)
F32 = jnp.float32
LOW = jnp.bfloat16
MESH_ID = pl.DeviceIdType.MESH


def dot_nn(left, right):
    return lax.dot_general(left, right, (((1,), (0,)), ((), ())), preferred_element_type=F32)


def dot_nt(left, right):
    return lax.dot_general(left, right, (((1,), (1,)), ((), ())), preferred_element_type=F32)


def dot_tn(left, right):
    return lax.dot_general(left, right, (((0,), (0,)), ((), ())), preferred_element_type=F32)


def standard(rows):
    centred = rows - jnp.mean(rows, axis=-1, keepdims=True)
    scale = lax.rsqrt(jnp.mean(centred * centred, axis=-1, keepdims=True) + NORM_EPS)
    return centred * scale, scale


def standard_back(grad, xhat, scale):
    inner = jnp.mean(grad * xhat, axis=-1, keepdims=True)
    return scale * (grad - jnp.mean(grad, axis=-1, keepdims=True) - xhat * inner)


def column_sum(rows):
    return jnp.sum(rows.astype(F32), axis=0, keepdims=True)


def relay_kernel(names, *refs):
    r = types.SimpleNamespace(**dict(zip(names, refs)))
    a, c, t = (lax.axis_index(name) for name in ("section", "seq", "tensor"))
    lines = lax.axis_size("section")
    chips = lax.axis_size("tensor")
    rows, buckets, width = r.inputs.shape[1:]
    half_width = width // 2
    local = rows * chips
    total = 2 * local
    stream_rows = local // STREAMS
    head_width = r.wo_in.shape[0]
    heads = head_width // HDIM
    blocks = local // QB
    units = r.wp_in.shape[0]
    scale = HDIM ** (-0.5)
    streams = range(STREAMS)

    def remote(src, dst, send, recv, **target):
        return pltpu.make_async_remote_copy(
            src_ref=src,
            dst_ref=dst,
            send_sem=send,
            recv_sem=recv,
            device_id=target,
            device_id_type=MESH_ID,
        )

    def drain(ref, sem):
        pltpu.make_async_copy(ref, ref, sem).wait()

    def row_block(index, size):
        return pl.ds(pl.multiple_of(index * size, size), size)

    near_chip = t + 1 - 2 * (t % 2)
    over_chip = (t + 2) % 4
    across_chip = 3 - t
    middle_chip = (t == 1) | (t == 2)
    end_chip = (t == 0) | (t == 3)
    owned = stream_rows // 2
    mine = row_block(t - 1, owned)
    my_half = row_block(c, local)

    r.kv[...] = jnp.zeros(r.kv.shape, LOW)

    barrier = pltpu.get_barrier_semaphore()
    greeted = 0
    for line in range(lines):
        for chip in range(chips):
            for core in range(2):
                if (line, chip, core) != (0, 0, 0) and (core == 0 or line * chip == 0):
                    there = {
                        "section": (a + line) % lines,
                        "seq": (c + core) % 2,
                        "tensor": (t + chip) % chips,
                    }
                    pl.semaphore_signal(barrier, inc=1, device_id=there, device_id_type=MESH_ID)
                    greeted += 1
    pl.semaphore_wait(barrier, greeted)

    def beside(s):
        return s + 1 - 2 * (s % 2)

    def above(s):
        return (s + 2) % 4

    def store(p):
        return (r.wq, r.wo, r.wf, r.wp)[p]

    def source(p):
        return (r.wq_in, r.wo_in, r.wf_in, r.wp_in)[p]

    def height(p):
        return source(p).shape[0]

    def core_half(p, s, core):
        return store(p).at[s, row_block(core, height(p) // 2)]

    def first_hop(p, s, neighbour, which):
        return remote(
            source(p).at[row_block(c, height(p) // 2)],
            core_half(p, s, c),
            r.w_first_s.at[p, which],
            r.w_first_r.at[s, p],
            section=neighbour,
        )

    def second_hop(p, s, which):
        view = store(p).at[s, row_block(2 * c + which, height(p) // 4)]
        return remote(
            view, view, r.w_second_s.at[s, p], r.w_second_r.at[s, p, which], section=3 - s
        )

    def core_hop(p, s, core):
        view = core_half(p, s, core)
        return remote(view, view, r.w_core_s.at[s, p], r.w_core_r.at[s, p], seq=1 - c)

    def own_copy(p):
        return pltpu.make_async_copy(source(p), store(p).at[a], r.w_own.at[p])

    def pass_on(s, p, which):
        line = (beside(s), above(s))[which]

        @pl.when(a == line)
        def _():
            first_hop(p, s, line, which).wait_recv()
            second_hop(p, s, which).start()
            core_hop(p, s, c).start()

    def pass_all(s, pieces):
        for p in pieces:
            for which in range(2):
                pass_on(s, p, which)

    def pass_far(s, p):
        @pl.when(a == 3 - s)
        def _():
            second_hop(p, s, 0).wait_recv()
            second_hop(p, s, 1).wait_recv()
            core_hop(p, s, c).start()

    def need(s, p):
        @pl.when(s == 0)
        def _():
            if p < 2:
                pass_all(0, (p,))
            pass_far(0, p)

        @pl.when(a == s)
        def _():
            own_copy(p).wait()

        @pl.when(a != s)
        def _():
            core_hop(p, s, 1 - c).wait_recv()

    def small_copy(step, line, slot):
        return remote(
            r.small_own, r.small.at[slot], r.small_s.at[step], r.small_r.at[slot], section=line
        )

    def count_copy(step, line, slot):
        return remote(
            r.count_own.at[line],
            r.count.at[slot],
            r.count_s.at[step],
            r.count_r.at[slot],
            section=line,
        )

    singles = (r.ln1_gain, r.ln1_shift, r.ln2_gain, r.ln2_shift, r.b_out, r.b_proj)
    for place, single in enumerate(singles):
        r.small_own[place : place + 1] = single[...]
    r.small_own[6:7, :units] = r.b_fc[...]
    r.small_own[7:8, :head_width] = r.b_qv[0:1]
    r.small_own[7:8, half_width : half_width + head_width] = r.b_qv[1:2]
    for step in range(1, lines):
        small_copy(step - 1, (a + step) % lines, a).start()
    for p in range(4):
        for which, line in enumerate((beside(a), above(a))):
            first_hop(p, a, line, which).start()
    for p in range(4):
        own_copy(p).start()
    r.small[a] = r.small_own[...]

    def iota(shape, dimension):
        return lax.broadcasted_iota(jnp.int32, shape, dimension)

    square = jnp.where(iota((KSEL, KSEL), 0) == iota((KSEL, KSEL), 1), 1.0, 0.0).astype(LOW)
    position = iota((KSEL, total), 1).astype(F32)
    for pair in range(lines * heads):
        line, head = pair // heads, pair % heads
        columns = dot_nt(square, r.chosen[pair].astype(F32).astype(LOW))
        for block in range(blocks):
            pick = head * blocks + block
            r.count_own[line, pick : pick + 1, :] = jnp.sum(
                jnp.where(columns[:, block : block + 1] == position, 1.0, 0.0),
                axis=0,
                keepdims=True,
            )
    for step in range(1, lines):
        count_copy(step - 1, (a + step) % lines, a).start()
    r.count[a] = r.count_own[a]

    NEAR, OVER, ACROSS = range(3)

    def gather(buffer, s, kind, j, owner, target, slot):
        view = buffer.at[s, j, row_block(owner - 1, owned)]
        return remote(
            view, view, r.ag_s.at[kind, j, slot], r.ag_r.at[kind, j, slot], tensor=target
        )

    def used_before(s, kind):
        return s > 0 if kind < 2 else s < lines - 1

    def gather_start(buffer, s, kind, j):
        @pl.when(used_before(s, kind))
        def _():
            gather_sent(buffer, s, kind, j)

        gather(buffer, s, kind, j, t, over_chip, OVER).start()
        gather(buffer, s, kind, j, t, across_chip, ACROSS).start()
        gather(buffer, s, kind, j, t, near_chip, NEAR).start()

    def gather_wait(buffer, s, kind, j):
        @pl.when(middle_chip)
        def _():
            gather(buffer, s, kind, j, across_chip, across_chip, ACROSS).wait_recv()

        @pl.when(end_chip)
        def _():
            gather(buffer, s, kind, j, near_chip, near_chip, NEAR).wait_recv()
            gather(buffer, s, kind, j, over_chip, over_chip, OVER).wait_recv()

    def gather_sent(buffer, s, kind, j):
        gather(buffer, s, kind, j, t, over_chip, OVER).wait_send()
        gather(buffer, s, kind, j, t, across_chip, ACROSS).wait_send()
        gather(buffer, s, kind, j, t, near_chip, NEAR).wait_send()

    def scatter(s, kind, j, owner, slot):
        return remote(
            r.part.at[kind, j, row_block(owner - 1, owned)],
            r.arrived.at[s, kind, j, slot],
            r.rs_s.at[kind, j, slot],
            r.rs_r.at[kind, j, slot],
            tensor=owner,
        )

    def scatter_start(s, kind, j, product):
        @pl.when(used_before(s, kind))
        def _():
            scatter_sent(s, kind, j)

        r.part[kind, j] = product.astype(LOW)

        @pl.when(end_chip)
        def _():
            scatter(s, kind, j, over_chip, OVER).start()
            scatter(s, kind, j, near_chip, NEAR).start()

        @pl.when(middle_chip)
        def _():
            scatter(s, kind, j, across_chip, ACROSS).start()

    def scatter_sum(s, kind, j):
        result = r.part[kind, j, mine].astype(F32)
        for slot in (NEAR, ACROSS, OVER):
            scatter(s, kind, j, t, slot).wait_recv()
            result = result + r.arrived[s, kind, j, slot].astype(F32)
        return result

    def scatter_sent(s, kind, j):
        @pl.when(end_chip)
        def _():
            scatter(s, kind, j, over_chip, OVER).wait_send()
            scatter(s, kind, j, near_chip, NEAR).wait_send()

        @pl.when(middle_chip)
        def _():
            scatter(s, kind, j, across_chip, ACROSS).wait_send()

    own_rows = (r.nrm, r.nmlp, r.ups, r.brn, r.act, r.gpre, r.mix, r.dqkv)
    all_rows = (
        r.all_nrm,
        r.all_nmlp,
        r.all_ups,
        r.all_brn,
        r.all_act,
        r.all_gpre,
        r.all_mix,
        r.all_dqkv,
    )

    def rows_copy(index, s, same, stays=False):
        core = c if same else 1 - c
        src = own_rows[index].at[s]
        dst = all_rows[index].at[a, c]
        if index <= BRN:
            src = src.at[:, :, row_block(core, half_width)]
        recv = r.heads_r.at[a] if index == DQKV else r.rows_r.at[index]
        if stays:
            return pltpu.make_async_copy(src, dst, recv)
        if same:
            return remote(src, dst, r.rows_s.at[index, s, 0], recv, section=s)
        return remote(src, dst, r.rows_s.at[index, s, 1], recv, section=s, seq=1 - c)

    passed_rows = {UPS: r.pass_ups, GPRE: r.pass_gpre}
    places = {UPS: 0, GPRE: 1}

    def detour_copy(index):
        return remote(
            own_rows[index].at[0],
            passed_rows[index],
            r.pass_s.at[places[index]],
            r.pass_r.at[places[index]],
            section=1,
        )

    def passed_copies(index):
        copies = []
        for step in range(2 if index <= BRN else 1):
            core = (c + step) % 2
            src = passed_rows[index]
            if index <= BRN:
                src = src.at[:, :, row_block(core, half_width)]
            send = r.pass_on_s.at[places[index], step]
            dst = all_rows[index].at[3, c]
            copies.append(remote(src, dst, send, r.rows_r.at[index], section=0, seq=core))
        return copies

    def pass_rows(index):
        @pl.when(a == 1)
        def _():
            detour_copy(index).wait_recv()
            for copy in passed_copies(index):
                copy.start()

    def goes_direct(index, s):
        return jnp.logical_not((a == 3) & (s == 0)) if index in passed_rows else a >= 0

    def rows_start(index, s):
        if index in passed_rows:

            @pl.when((a == 3) & (s == 0))
            def _():
                detour_copy(index).start()

        @pl.when(a == s)
        def _():
            rows_copy(index, s, True, True).start()

        @pl.when((a != s) & goes_direct(index, s))
        def _():
            rows_copy(index, s, True).start()

        if index <= BRN:

            @pl.when(goes_direct(index, s))
            def _():
                rows_copy(index, s, False).start()

    def forward_rows(s):
        for index in (NRM, MIX, NMLP, ACT):
            rows_start(index, s)

    def rows_sent(index, s):
        @pl.when((a != s) & goes_direct(index, s))
        def _():
            rows_copy(index, s, True).wait_send()

        if index <= BRN:

            @pl.when(goes_direct(index, s))
            def _():
                rows_copy(index, s, False).wait_send()

    def share_copy(index, core):
        view = all_rows[index].at[:, core]
        return remote(view, view, r.share_s.at[index - ACT], r.share_r.at[index - ACT], seq=1 - c)

    def share_heads(line, core):
        view = r.all_dqkv.at[line, core]
        return remote(view, view, r.heads_s.at[line], r.heads_sr.at[line], seq=1 - c)

    def share(index):
        drain(all_rows[index].at[:, c], r.rows_r.at[index])
        share_copy(index, c).start()

    def norm_copy(s):
        return remote(
            r.norm_part.at[s], r.norm_all.at[a], r.norm_s.at[s], r.norm_r, section=s
        )

    def norm_start(s):
        @pl.when(a == s)
        def _():
            pltpu.make_async_copy(r.norm_part.at[s], r.norm_all.at[a], r.norm_r).start()

        @pl.when(a != s)
        def _():
            norm_copy(s).start()

    def home_copy(what, s, j):
        src, dst, send, recv = what
        chip = 2 * j + t - 1
        return remote(src.at[s, j], dst.at[a], send.at[s, j], recv, section=s, tensor=chip)

    def home_start(what, s):
        @pl.when(middle_chip)
        def _():
            for j in streams:
                home_copy(what, s, j).start()

    def home_sent(what, s):
        @pl.when(middle_chip)
        def _():
            for j in streams:
                home_copy(what, s, j).wait_send()

    out_home = (r.out_low, r.acts, r.out_s, r.out_r)
    grad_home = (r.grad_low, r.grads, r.grad_s, r.grad_r)

    length = r.lengths[a // buckets, a % buckets]
    key = iota((stream_rows, total), 1)
    for j in streams:
        query = c * local + j * stream_rows + iota((stream_rows, total), 0)
        r.near[j] = jnp.where((query >= key) & (query - key < WIN), 1.0, 0.0)
    key_row = iota((1, total), 1)

    def row_mask(place):
        return jnp.where(place < length, 1.0, 0.0)

    def stream_mask(j):
        return row_mask(c * local + j * stream_rows + iota((stream_rows, 1), 0))

    def multiplicity(s, j, head):
        block = j * stream_rows // QB
        pick = head * blocks + block
        limit = (c * blocks + block) * QB - WIN
        return r.near[j] + jnp.where(key_row <= limit, r.count[s, pick : pick + 1, :], 0.0)

    def head_cols(head):
        return slice(head * HDIM, (head + 1) * HDIM)

    def kv_copy(s, j):
        view = r.kv.at[s, :, j * stream_rows : (j + 1) * stream_rows]
        return remote(view, view, r.kv_s.at[s, j], r.kv_r.at[s, j], seq=1 - c)

    def dkv_copy(s):
        return remote(r.dkv_out.at[s], r.dkv_in.at[s], r.dkv_s.at[s], r.dkv_r.at[s], seq=1 - c)

    def own_sequence(ref):
        both = ref[a // buckets].astype(F32)
        picked = both[:, 0, :]
        for bucket in range(1, buckets):
            picked = jnp.where(a % buckets == bucket, both[:, bucket, :], picked)
        return picked

    def first_copy(stream):
        return remote(
            r.first_out, r.first_in.at[stream], r.first_s, r.first_r.at[stream], tensor=1 + t % 2
        )

    own_place = c * local + t * rows + iota((rows, 1), 0)
    r.first_out[0] = own_sequence(r.inputs).astype(LOW)
    r.first_out[1] = (own_sequence(r.cotangent) * row_mask(own_place)).astype(LOW)
    first_copy(t // 2).start()
    r.norm_part[...] = jnp.zeros_like(r.norm_part)

    def first_rows(j):
        @pl.when(middle_chip)
        def _():
            first_copy(j).wait_recv()
            r.hidden[j] = r.first_in[j, 0].astype(F32)
            r.upstream[j] = r.first_in[j, 1]

    def on_owner(stage):
        def run(s, j):
            @pl.when(middle_chip)
            def _():
                stage(s, j)

        return run

    @on_owner
    def enter(s, j):
        xhat, inverse = standard(r.hidden[j])
        r.xhat1[s, j] = xhat
        r.inv1[s, j] = jnp.broadcast_to(inverse, (owned, 128))
        r.nrm[s, j, mine] = (xhat * r.small[s, 0:1] + r.small[s, 1:2]).astype(LOW)
        gather_start(r.nrm, s, 0, j)

    def project(s, j):
        gather_wait(r.nrm, s, 0, j)
        normed = r.nrm[s, j]
        place = row_block(c * STREAMS + j, stream_rows)
        bias_v = r.small[s, 7:8, half_width : half_width + head_width]
        key_rows = dot_nt(normed, r.wq[s, head_width : 2 * head_width])
        value_rows = dot_nt(normed, r.wq[s, 2 * head_width : 3 * head_width]) + bias_v
        r.kv[s, 0, place] = key_rows.astype(LOW)
        r.kv[s, 1, place] = value_rows.astype(LOW)

    def ask(s, j):
        queries = dot_nt(r.nrm[s, j], r.wq[s, 0:head_width]) + r.small[s, 7:8, :head_width]
        r.qry[s, j] = queries.astype(LOW)

    def attend_line(s, j):
        mixed = []
        for head in range(heads):
            cols = head_cols(head)
            times = multiplicity(s, j, head)
            scores = scale * dot_nt(r.qry[s, j, :, cols], r.kv[s, 0, :, cols])
            scores = jnp.where(times > 0.0, scores, MASKED)
            top = jnp.max(scores, axis=-1, keepdims=True)
            terms = times * jnp.exp(scores - top)
            weights = terms / jnp.sum(terms, axis=-1, keepdims=True)
            r.soft[s, j, head] = weights
            mixed.append(dot_nn(weights.astype(LOW), r.kv[s, 1, :, cols]))
        r.mix[s, j] = (jnp.concatenate(mixed, axis=-1) * stream_mask(j)).astype(LOW)

    def leave_attention(s, j):
        scatter_start(s, 0, j, dot_nn(r.mix[s, j], r.wo[s]))

    @on_owner
    def between(s, j):
        middle = r.hidden[j] + scatter_sum(s, 0, j) + r.small[s, 4:5]
        r.middle[j] = middle
        xhat, inverse = standard(middle)
        r.xhat2[s, j] = xhat
        r.inv2[s, j] = jnp.broadcast_to(inverse, (owned, 128))
        r.nmlp[s, j, mine] = (xhat * r.small[s, 2:3] + r.small[s, 3:4]).astype(LOW)
        gather_start(r.nmlp, s, 1, j)

    def feed(s, j):
        gather_wait(r.nmlp, s, 1, j)
        before = dot_nn(r.nmlp[s, j], r.wf[s]) + r.small[s, 6:7, :units]
        bend = jnp.tanh(0.7978845608028654 * (before + 0.044715 * before * before * before))
        r.act[s, j] = (0.5 * before * (1.0 + bend)).astype(LOW)
        r.slope[s, j] = 0.5 * (1.0 + bend) + 0.5 * before * (1.0 - bend * bend) * (
            0.7978845608028654 * (1.0 + 3 * 0.044715 * before * before)
        )


    def leave_feed(s, j):
        scatter_start(s, 1, j, dot_nn(r.act[s, j], r.wp[s]))

    @on_owner
    def finish(s, j):
        result = r.middle[j] + scatter_sum(s, 1, j) + r.small[s, 5:6]
        r.out_low[s, j] = result.astype(LOW)
        r.hidden[j] = result.astype(LOW).astype(F32)

    def small_ready(s):
        @pl.when(a != s)
        def _():
            small_copy(0, a, s).wait_recv()

    small_ready(0)
    for j in streams:
        first_rows(j)
        enter(0, j)

    def forward(s, _):
        need(s, 0)
        need(s, 1)

        @pl.when(a != s)
        def _():
            count_copy(0, a, s).wait_recv()

        for j in streams:
            project(s, j)

            @pl.when(c == 0)
            def _():
                kv_copy(s, j).start()

            ask(s, j)
            if j == 0:

                @pl.when(c == 1)
                def _():
                    for other in streams:
                        kv_copy(s, other).wait_recv()

            if j == STREAMS - 1:

                @pl.when(s == 0)
                def _():
                    pass_all(0, (2,))

            attend_line(s, j)
            leave_attention(s, j)

        @pl.when(s == 0)
        def _():
            pass_all(0, (3,))
            for later in range(1, lines):
                pass_all(later, (0, 1, 2))

        @pl.when(s == 1)
        def _():
            pass_far(1, 2)
            pass_far(1, 3)
            for later in range(2, lines):
                for p in range(4):
                    pass_far(later, p)

        for j in streams:
            between(s, j)
        @pl.when(s == 0)
        def _():
            for later in range(1, lines):
                pass_all(later, (3,))

        need(s, 2)
        for j in streams:
            feed(s, j)
            if j == 0:
                need(s, 3)
            leave_feed(s, j)


        @pl.when(s >= 2)
        def _():
            forward_rows(s - 2)


        @pl.when(s + 1 < lines)
        def _():
            small_ready(s + 1)

        for j in streams:
            finish(s, j)

            @pl.when(s + 1 < lines)
            def _():
                enter(s + 1, j)

        home_start(out_home, s)

        @pl.when(s == 0)
        def _():
            pass_far(1, 0)
            pass_far(1, 1)

        return 0

    lax.fori_loop(0, lines, forward, 0)

    @on_owner
    def turn(s, j):
        upstream = r.upstream[j]
        r.ups[s, j, mine] = upstream
        gather_start(r.ups, s, 2, j)
        r.norm_part[s, 5:6] += column_sum(upstream)

    def feed_back(s, j):
        gather_wait(r.ups, s, 2, j)
        grad_pre = (dot_nt(r.ups[s, j], r.wp[s]) * r.slope[s, j]).astype(LOW)
        r.gpre[s, j] = grad_pre
        scatter_start(s, 2, j, dot_nt(grad_pre, r.wf[s]))
        r.norm_part[s, 6:7, :units] += column_sum(grad_pre)

    @on_owner
    def between_back(s, j):
        grad = scatter_sum(s, 2, j)
        xhat = r.xhat2[s, j]
        upstream = r.upstream[j].astype(F32)
        grad_middle = upstream + standard_back(
            grad * r.small[s, 2:3], xhat, r.inv2[s, j, :, 0:1]
        )
        r.middle[j] = grad_middle
        branch = grad_middle.astype(LOW)
        r.brn[s, j, mine] = branch
        gather_start(r.brn, s, 3, j)
        r.norm_part[s, 2:3] += column_sum(grad * xhat)
        r.norm_part[s, 3:4] += column_sum(grad)
        r.norm_part[s, 4:5] += column_sum(branch)

    def mixed_back(s, j):
        gather_wait(r.brn, s, 3, j)
        r.gmix[j] = (dot_nt(r.brn[s, j], r.wo[s]) * stream_mask(j)).astype(LOW)

    def attend_line_back(s, j):
        grad_q, grad_k, grad_v = [], [], []
        for head in range(heads):
            cols = head_cols(head)
            weights = r.soft[s, j, head]
            grad_head = r.gmix[j, :, cols]
            grad_weights = dot_nt(grad_head, r.kv[s, 1, :, cols])
            inner = jnp.sum(weights * grad_weights, axis=-1, keepdims=True)
            grad_scores = (weights * (grad_weights - inner)).astype(LOW)
            grad_k.append(scale * dot_tn(grad_scores, r.qry[s, j, :, cols]))
            grad_v.append(dot_tn(weights.astype(LOW), grad_head))
            grad_q.append(scale * dot_nn(grad_scores, r.kv[s, 0, :, cols]))
        for which, grad in enumerate((grad_k, grad_v)):
            grad = jnp.concatenate(grad, axis=-1)
            r.dkv_all[which] = grad if j == STREAMS - 1 else r.dkv_all[which] + grad
        grad_q = jnp.concatenate(grad_q, axis=-1).astype(LOW)
        r.dqkv[s, 0, j] = grad_q
        r.norm_part[s, 7:8, :head_width] += column_sum(grad_q)

    def join_keys(s, j):
        for which in range(2):
            joined = r.dkv_all[which, row_block(c * STREAMS + j, stream_rows)].astype(LOW)
            r.dqkv[s, 1 + which, j] = joined
            if which == 1:
                lanes = slice(half_width, half_width + head_width)
                r.norm_part[s, 7:8, lanes] += column_sum(joined)

    def leave_back(s, j):
        product = dot_nn(r.dqkv[s, 0, j], r.wq[s, 0:head_width])
        for which in range(1, 3):
            weight = r.wq[s, which * head_width : (which + 1) * head_width]
            product = product + dot_nn(r.dqkv[s, which, j], weight)
        scatter_start(s, 3, j, product)

    @on_owner
    def finish_back(s, j):
        grad = scatter_sum(s, 3, j)
        xhat = r.xhat1[s, j]
        result = r.middle[j] + standard_back(
            grad * r.small[s, 0:1], xhat, r.inv1[s, j, :, 0:1]
        )
        r.upstream[j] = result.astype(LOW)
        r.grad_low[s, j] = result.astype(LOW)
        r.norm_part[s, 0:1] += column_sum(grad * xhat)
        r.norm_part[s, 1:2] += column_sum(grad)

    last_first = tuple(reversed(streams))
    for j in last_first:
        turn(lines - 1, j)

    def backward(index, _):
        s = lines - 1 - index
        for j in last_first:
            feed_back(s, j)
        rows_start(UPS, s)
        rows_start(GPRE, s)

        @pl.when(index < 2)
        def _():
            forward_rows(lines - 2 + index)

        @pl.when(index == lines - 1)
        def _():
            share(ACT)
            share(MIX)

        for j in last_first:
            between_back(s, j)
        for j in last_first:
            mixed_back(s, j)
            if j == 0:
                rows_start(BRN, s)
            attend_line_back(s, j)

            @pl.when(c == 1)
            def _():
                join_keys(s, j)
                leave_back(s, j)

        @pl.when(c == 1)
        def _():
            r.dkv_out[s] = r.dkv_all[:, 0:local].astype(LOW)
            dkv_copy(s).start()

        @pl.when(c == 0)
        def _():
            dkv_copy(s).wait_recv()
            r.dkv_all[:, 0:local] += r.dkv_in[s].astype(F32)
            for j in last_first:
                join_keys(s, j)
                leave_back(s, j)

        rows_start(DQKV, s)

        @pl.when(s == 0)
        def _():
            pass_rows(UPS)
            pass_rows(GPRE)

        for j in last_first:
            finish_back(s, j)

            @pl.when(s > 0)
            def _():
                turn(s - 1, j)

        norm_start(s)
        home_start(grad_home, s)
        return 0

    lax.fori_loop(0, lines, backward, 0)

    share(GPRE)

    drain(r.norm_all, r.norm_r)
    slot = c * chips + t
    norm_sum = r.norm_all[0]
    for line in range(1, lines):
        norm_sum = norm_sum + r.norm_all[line]
    r.ends[slot] = norm_sum

    def ends_copy(step):
        core, chip = step // chips, step % chips
        view = r.ends.at[slot]
        return remote(
            view,
            view,
            r.ends_s.at[step - 1],
            r.ends_r,
            seq=(c + core) % 2,
            tensor=(t + chip) % chips,
        )

    for step in range(1, 2 * chips):
        ends_copy(step).start()

    for line in range(lines):
        drain(r.all_dqkv.at[line, c], r.heads_r.at[line])
        share_heads(line, c).start()

    for index in (UPS, GPRE):

        @pl.when(a == 3)
        def _():
            detour_copy(index).wait_send()

        @pl.when(a == 1)
        def _():
            for copy in passed_copies(index):
                copy.wait_send()

    for kind, buffer in enumerate((r.nrm, r.nmlp, r.ups, r.brn)):
        for j in streams:
            scatter_sent(0, kind, j)

            @pl.when(middle_chip)
            def _():
                gather_sent(buffer, 0, kind, j)

    for index in range(ACT):
        drain(all_rows[index], r.rows_r.at[index])
    for index in range(ACT, DQKV):
        share_copy(index, 1 - c).wait_recv()
        share_copy(index, c).wait_send()
    for line in range(lines):
        share_heads(line, 1 - c).wait_recv()
        share_heads(line, c).wait_send()
    drain(r.acts, r.out_r)
    drain(r.grads, r.grad_r)
    drain(r.ends.at[0 : 2 * chips - 1], r.ends_r)
    for step in range(1, 2 * chips):
        ends_copy(step).wait_send()
    for step in range(1, lines):
        small_copy(step - 1, (a + step) % lines, a).wait_send()
        count_copy(step - 1, (a + step) % lines, a).wait_send()
    for p in range(4):
        for which, line in enumerate((beside(a), above(a))):
            first_hop(p, a, line, which).wait_send()

    first_copy(t // 2).wait_send()

    def sent(s, _):
        home_sent(out_home, s)
        home_sent(grad_home, s)

        @pl.when(a != s)
        def _():
            norm_copy(s).wait_send()

        @pl.when(c == 0)
        def _():
            for j in streams:
                kv_copy(s, j).wait_send()

        @pl.when(c == 1)
        def _():
            dkv_copy(s).wait_send()

        for index in range(8):
            rows_sent(index, s)
        for p in range(4):

            @pl.when((a == beside(s)) | (a == above(s)))
            def _():
                second_hop(p, s, 0).wait_send()

            @pl.when(a != s)
            def _():
                core_hop(p, s, c).wait_send()

        return 0

    lax.fori_loop(0, lines, sent, 0)


def relay_call(inputs, cotangent, lengths, chosen, singles, weights):
    lines = lax.axis_size("section")
    chips = lax.axis_size("tensor")
    rows, buckets, width = inputs.shape[1:]
    local, total, half = rows * chips, 2 * rows * chips, width // 2
    head_width, units = weights["wo_in"].shape[0], weights["wp_in"].shape[0]
    heads = head_width // HDIM
    stream = local // STREAMS
    peers, owned = chips - 1, stream // 2
    vmem, dma = pltpu.VMEM, pltpu.SemaphoreType.DMA
    operands = dict(
        inputs=inputs,
        cotangent=cotangent,
        lengths=lengths,
        chosen=chosen,
        **singles,
        **weights,
    )

    def space(name):
        if name in weights:
            return pl.ANY
        return pltpu.SMEM if operands[name] is lengths else pltpu.VMEM

    sums = dict(
        acts=((lines, rows, width), LOW),
        grads=((lines, rows, width), LOW),
        ends=((2 * chips, 8, width), F32),
    )
    gathered = dict(
        all_nrm=((lines, 2, STREAMS, stream, half), LOW),
        all_nmlp=((lines, 2, STREAMS, stream, half), LOW),
        all_ups=((lines, 2, STREAMS, stream, half), LOW),
        all_brn=((lines, 2, STREAMS, stream, half), LOW),
        all_act=((lines, 2, STREAMS, stream, units), LOW),
        all_gpre=((lines, 2, STREAMS, stream, units), LOW),
        all_mix=((lines, 2, STREAMS, stream, head_width), LOW),
        all_dqkv=((lines, 2, 3, STREAMS, stream, head_width), LOW),
    )
    outputs = dict(**sums, **gathered)
    scratch = dict(
        wq=vmem((lines,) + weights["wq_in"].shape, LOW),
        wo=vmem((lines,) + weights["wo_in"].shape, LOW),
        wf=vmem((lines,) + weights["wf_in"].shape, LOW),
        wp=vmem((lines,) + weights["wp_in"].shape, LOW),
        small_own=vmem((8, width), F32),
        small=vmem((lines, 8, width), F32),
        count_own=vmem((lines, 8, total), F32),
        count=vmem((lines, 8, total), F32),
        hidden=vmem((STREAMS, owned, width), F32),
        middle=vmem((STREAMS, owned, width), F32),
        upstream=vmem((STREAMS, owned, width), LOW),
        first_out=vmem((2, owned, width), LOW),
        first_in=vmem((STREAMS, 2, owned, width), LOW),
        xhat1=vmem((lines, STREAMS, owned, width), F32),
        inv1=vmem((lines, STREAMS, owned, 128), F32),
        xhat2=vmem((lines, STREAMS, owned, width), F32),
        inv2=vmem((lines, STREAMS, owned, 128), F32),
        nrm=vmem((lines, STREAMS, stream, width), LOW),
        nmlp=vmem((lines, STREAMS, stream, width), LOW),
        ups=vmem((lines, STREAMS, stream, width), LOW),
        brn=vmem((lines, STREAMS, stream, width), LOW),
        act=vmem((lines, STREAMS, stream, units), LOW),
        gpre=vmem((lines, STREAMS, stream, units), LOW),
        slope=vmem((lines, STREAMS, stream, units), F32),
        mix=vmem((lines, STREAMS, stream, head_width), LOW),
        qry=vmem((lines, STREAMS, stream, head_width), LOW),
        gmix=vmem((STREAMS, stream, head_width), LOW),
        dqkv=vmem((lines, 3, STREAMS, stream, head_width), LOW),
        pass_ups=vmem((STREAMS, stream, width), LOW),
        pass_gpre=vmem((STREAMS, stream, units), LOW),
        kv=vmem((lines, 2, total, head_width), LOW),
        soft=vmem((lines, STREAMS, heads, stream, total), F32),
        near=vmem((STREAMS, stream, total), F32),
        dkv_all=vmem((2, total, head_width), F32),
        dkv_out=vmem((lines, 2, local, head_width), LOW),
        dkv_in=vmem((lines, 2, local, head_width), LOW),
        part=vmem((4, STREAMS, stream, width), LOW),
        arrived=vmem((lines, 4, STREAMS, peers, owned, width), LOW),
        out_low=vmem((lines, STREAMS, owned, width), LOW),
        grad_low=vmem((lines, STREAMS, owned, width), LOW),
        norm_part=vmem((lines, 8, width), F32),
        norm_all=vmem((lines, 8, width), F32),
        w_first_s=dma((4, 2)),
        w_first_r=dma((lines, 4)),
        w_second_s=dma((lines, 4)),
        w_second_r=dma((lines, 4, 2)),
        w_core_s=dma((lines, 4)),
        w_core_r=dma((lines, 4)),
        w_own=dma((4,)),
        small_s=dma((lines - 1,)),
        small_r=dma((lines,)),
        count_s=dma((lines - 1,)),
        count_r=dma((lines,)),
        ag_s=dma((4, STREAMS, peers)),
        ag_r=dma((4, STREAMS, peers)),
        rs_s=dma((4, STREAMS, peers)),
        rs_r=dma((4, STREAMS, peers)),
        kv_s=dma((lines, STREAMS)),
        kv_r=dma((lines, STREAMS)),
        dkv_s=dma((lines,)),
        dkv_r=dma((lines,)),
        rows_s=dma((8, lines, 2)),
        rows_r=dma((8,)),
        pass_s=dma((2,)),
        pass_r=dma((2,)),
        pass_on_s=dma((2, 2)),
        share_s=dma((4,)),
        share_r=dma((4,)),
        heads_r=dma((lines,)),
        heads_s=dma((lines,)),
        heads_sr=dma((lines,)),
        first_s=dma,
        first_r=dma((STREAMS,)),
        out_s=dma((lines, STREAMS)),
        out_r=dma,
        grad_s=dma((lines, STREAMS)),
        grad_r=dma,
        norm_s=dma((lines,)),
        norm_r=dma,
        ends_s=dma((2 * chips - 1,)),
        ends_r=dma,
    )
    names = tuple(operands) + tuple(outputs) + tuple(scratch)
    results = pl.pallas_call(
        functools.partial(relay_kernel, names),
        out_shape=[jax.ShapeDtypeStruct(shape, kind) for shape, kind in outputs.values()],
        in_specs=[pl.BlockSpec(memory_space=space(name)) for name in operands],
        out_specs=[
            pl.BlockSpec(memory_space=pl.ANY if name in gathered else pltpu.VMEM)
            for name in outputs
        ],
        scratch_shapes=list(scratch.values()),
        compiler_params=pltpu.CompilerParams(
            collective_id=0, has_side_effects=True, vmem_limit_bytes=60 * 2**20
        ),
        name="relay",
    )(*operands.values())
    return dict(zip(outputs, results))


def weights_kernel(names, *refs):
    r = types.SimpleNamespace(**dict(zip(names, refs)))
    micro_count, rows, buckets, width = r.activations.shape
    chips, units, head_width = r.ends.shape[0] // 2, r.all_act.shape[-1], r.all_mix.shape[-1]
    lines = r.acts.shape[0]
    loads = [
        pltpu.make_async_copy(source, target, r.load_sem.at[place])
        for place, (source, target) in enumerate(
            (
                (r.all_act, r.act),
                (r.all_ups, r.ups),
                (r.all_nmlp, r.nmlp),
                (r.all_gpre, r.gpre),
                (r.all_mix, r.mix),
                (r.all_brn, r.brn),
                (r.all_nrm, r.nrm),
                (r.all_dqkv, r.dqkv),
            )
        )
    ]
    stores = [
        pltpu.make_async_copy(source, target, r.store_sem.at[place])
        for place, (source, target) in enumerate(
            (
                (r.own_proj, r.w_proj),
                (r.own_fc, r.w_fc),
                (r.own_out, r.w_out),
                (r.own_qkv, r.w_qkv),
            )
        )
    ]
    for load in loads:
        load.start()

    sums = r.ends[0]
    for other in range(1, 2 * chips):
        sums = sums + r.ends[other]
    singles = (r.ln1_gain, r.ln1_shift, r.ln2_gain, r.ln2_shift, r.b_out, r.b_proj)
    for place, single in enumerate(singles):
        single[...] = sums[place : place + 1]
    for chip in range(chips):
        both = r.ends[chip] + r.ends[chips + chip]
        r.b_fc[:, chip * units : (chip + 1) * units] = both[6:7, :units]
        here = slice(chip * head_width, (chip + 1) * head_width)
        r.b_qv[0:1, here] = both[7:8, :head_width]
        r.b_qv[1:2, here] = both[7:8, width // 2 : width // 2 + head_width]
    for target, source in ((r.activations, r.acts), (r.in_grads, r.grads)):
        for micro in range(micro_count):
            rows_of = [
                source[micro * buckets + bucket].astype(F32)[:, None, :]
                for bucket in range(buckets)
            ]
            target[micro] = jnp.concatenate(rows_of, axis=1).astype(LOW)

    def flat(array):
        return array.reshape(lines * 2 * chips * rows, array.shape[-1])

    loads[0].wait()
    loads[1].wait()
    r.own_proj[...] = dot_tn(flat(r.act[...]), flat(r.ups[...]))
    stores[0].start()
    loads[2].wait()
    loads[3].wait()
    r.own_fc[...] = dot_tn(flat(r.nmlp[...]), flat(r.gpre[...]))
    stores[1].start()
    loads[4].wait()
    loads[5].wait()
    r.own_out[...] = dot_tn(flat(r.mix[...]), flat(r.brn[...]))
    stores[2].start()
    loads[6].wait()
    loads[7].wait()
    nrm = flat(r.nrm[...])
    for which in range(3):
        r.own_qkv[which] = dot_tn(flat(r.dqkv[:, :, which]), nrm)
    stores[3].start()
    for store in stores:
        store.wait()


def weights_call(relayed, inputs_shape, head_width, units):
    chips = lax.axis_size("tensor")
    width = inputs_shape[-1]
    half = width // 2
    outputs = dict(
        activations=(inputs_shape, LOW),
        in_grads=(inputs_shape, LOW),
        ln1_gain=((1, width), F32),
        ln1_shift=((1, width), F32),
        w_qkv=((3, head_width, half), F32),
        b_qv=((2, width), F32),
        w_out=((head_width, half), F32),
        b_out=((1, width), F32),
        ln2_gain=((1, width), F32),
        ln2_shift=((1, width), F32),
        w_fc=((half, units), F32),
        b_fc=((1, chips * units), F32),
        w_proj=((units, half), F32),
        b_proj=((1, width), F32),
    )
    rows = ("act", "ups", "nmlp", "gpre", "mix", "brn", "nrm", "dqkv")
    own = dict(own_proj="w_proj", own_fc="w_fc", own_out="w_out", own_qkv="w_qkv")
    scratch = {name: pltpu.VMEM(relayed["all_" + name].shape, LOW) for name in rows}
    scratch.update({name: pltpu.VMEM(outputs[of][0], F32) for name, of in own.items()})
    scratch["load_sem"] = pltpu.SemaphoreType.DMA((8,))
    scratch["store_sem"] = pltpu.SemaphoreType.DMA((4,))
    whole, apart = pl.BlockSpec(memory_space=pltpu.VMEM), pl.BlockSpec(memory_space=pl.ANY)
    small = ("acts", "grads", "ends")
    return pl.pallas_call(
        functools.partial(weights_kernel, tuple(relayed) + tuple(outputs) + tuple(scratch)),
        out_shape=[jax.ShapeDtypeStruct(shape, kind) for shape, kind in outputs.values()],
        in_specs=[whole if name in small else apart for name in relayed],
        out_specs=[apart if name in own.values() else whole for name in outputs],
        scratch_shapes=list(scratch.values()),
        compiler_params=pltpu.CompilerParams(vmem_limit_bytes=60 * 2**20),
        name="weight_gradients",
    )(*relayed.values())


def on_line(
    inputs,
    cotangent,
    lengths,
    chosen,
    ln1_gain,
    ln1_shift,
    w_qkv,
    b_qv,
    w_out,
    b_out,
    ln2_gain,
    ln2_shift,
    w_fc,
    b_fc,
    w_proj,
    b_proj,
):
    head_width, units = w_out.shape[1], w_fc.shape[2]
    singles = dict(
        ln1_gain=ln1_gain,
        ln1_shift=ln1_shift,
        ln2_gain=ln2_gain,
        ln2_shift=ln2_shift,
        b_out=b_out,
        b_proj=b_proj,
        b_fc=b_fc,
        b_qv=b_qv[0],
    )
    weights = dict(
        wq_in=jnp.swapaxes(w_qkv[0], 1, 2).reshape(-1, inputs.shape[-1]),
        wo_in=w_out[0],
        wf_in=w_fc[0],
        wp_in=w_proj[0],
    )
    picks = chosen.reshape((-1,) + chosen.shape[-2:])
    relayed = relay_call(inputs, cotangent, lengths, picks, singles, weights)
    results = list(weights_call(relayed, inputs.shape, head_width, units))
    results[4] = jnp.swapaxes(results[4], 1, 2)
    vectors = (2, 3, 7, 8, 9, 11, 13)
    return tuple(
        result if place in vectors else result[None] for place, result in enumerate(results)
    )


def fits_lines(mesh):
    return mesh.shape["section"] == 4 and mesh.shape["seq"] == 2 and mesh.shape["tensor"] == 4


def solution(mesh):
    placed = (
        P(None, ("seq", "tensor"), None, None),
        P(None, ("seq", "tensor"), None, None),
        P(),
        P("section", None, None, "tensor", "seq", None),
        P("section", None),
        P("section", None),
        P("section", None, None, "tensor"),
        P("section", None, "tensor"),
        P("section", "tensor", None),
        P("section", None),
        P("section", None),
        P("section", None),
        P("section", None, "tensor"),
        P("section", "tensor"),
        P("section", "tensor", None),
        P("section", None),
    )
    return jax.shard_map(
        on_line if fits_lines(mesh) else on_device,
        mesh=mesh,
        in_specs=placed,
        out_specs=(
            P("section", None, ("seq", "tensor"), None, None),
            P("section", None, ("seq", "tensor"), None, None),
            P("section", None),
            P("section", None),
            P("section", None, "seq", "tensor"),
            P("section", None, None),
            P("section", "tensor", "seq"),
            P("section", None),
            P("section", None),
            P("section", None),
            P("section", "seq", "tensor"),
            P("section", None),
            P("section", "tensor", "seq"),
            P("section", None),
        ),
        check_vma=False,
    )
```

```python
import functools
import types

import jax
import jax.numpy as jnp
from jax import lax
from jax.experimental import pallas as pl
from jax.experimental.pallas import tpu as pltpu
from jax.sharding import PartitionSpec as P

HDIM = 64
WIN = 64
QB = 64
KSEL = 64


NORM_EPS = 1e-05
MASKED = -1000000000.0


def from_behind(value, axis, steps):
    count = lax.axis_size(axis)
    first, last = (max(0, -steps), min(count, count - steps))
    return lax.ppermute(value, axis, [(source, source + steps) for source in range(first, last)])


def layer_norm(values, gain, shift):
    average = jnp.mean(values, axis=-1, keepdims=True)
    centred = values - average
    variance = jnp.mean(centred * centred, axis=-1, keepdims=True)
    return centred * lax.rsqrt(variance + NORM_EPS) * gain + shift


def gelu_tanh(values):
    return (
        0.5
        * values
        * (1.0 + jnp.tanh(0.7978845608028654 * (values + 0.044715 * values * values * values)))
    )


def gather_rows(row_block):
    return lax.all_gather(row_block, "tensor", axis=0, tiled=True)


def scatter_product(left_rows, weight, formula):
    return lax.psum_scatter(
        jnp.einsum(formula, left_rows, weight, preferred_element_type=jnp.float32).astype(
            jnp.bfloat16
        ),
        "tensor",
        scatter_dimension=0,
        tiled=True,
    ).astype(jnp.float32)


def near_slabs(full_rows, seq_start, seq_first, length_local):
    buckets = full_rows.shape[1]
    heads_local = full_rows.shape[2] // HDIM
    blocks = length_local // QB
    earlier = lax.dynamic_slice_in_dim(full_rows, jnp.maximum(seq_start - WIN, 0), WIN, 0)
    earlier = jnp.where(seq_first, jnp.zeros_like(earlier), earlier)
    local_part = lax.dynamic_slice_in_dim(full_rows, seq_start, length_local, 0)
    segment = jnp.concatenate([earlier, local_part], 0).reshape(
        length_local + WIN, buckets, heads_local, HDIM
    )
    return jnp.concatenate(
        [
            segment[offset_index * QB : offset_index * QB + length_local].reshape(
                blocks, QB, buckets, heads_local, HDIM
            )
            for offset_index in range(WIN // QB + 1)
        ],
        1,
    )


def far_rows(full_rows, flat_index):
    total_rows, buckets, feature_width = full_rows.shape
    heads_local = feature_width // HDIM
    return jnp.take(full_rows.reshape(total_rows * buckets * heads_local, HDIM), flat_index, axis=0)


def key_geometry(chosen_now, seq_start, blocks):
    buckets, heads_local = (chosen_now.shape[0], chosen_now.shape[1])
    bucket_ids = lax.broadcasted_iota(jnp.int32, chosen_now.shape, 0)
    head_ids = lax.broadcasted_iota(jnp.int32, chosen_now.shape, 1)
    flat_index = (chosen_now * buckets + bucket_ids) * heads_local + head_ids
    block_start = seq_start + QB * lax.broadcasted_iota(jnp.int32, (blocks, 1, 1), 0)
    query_ids = lax.broadcasted_iota(jnp.int32, (1, QB, 1), 1)
    key_ids = lax.broadcasted_iota(jnp.int32, (1, 1, WIN + QB), 2)
    distance = query_ids + WIN - key_ids
    near_ok = (distance >= 0) & (distance < WIN) & (block_start + key_ids - WIN >= 0)
    far_ok = chosen_now + WIN <= block_start.reshape(1, 1, blocks, 1)
    near_mask = jnp.broadcast_to(
        near_ok[:, None, None], (blocks, buckets, heads_local, QB, WIN + QB)
    )
    far_mask = jnp.broadcast_to(
        jnp.transpose(far_ok, (2, 0, 1, 3))[:, :, :, None, :],
        (blocks, buckets, heads_local, QB, KSEL),
    )
    return (flat_index, jnp.concatenate([near_mask, far_mask], -1))


def attention_setup(queries, key_rows, value_rows, chosen_now, seq_start, seq_first):
    length_local, buckets, feature_width = queries.shape
    heads_local = feature_width // HDIM
    blocks = length_local // QB
    query_blocks = queries.reshape(blocks, QB, buckets, heads_local, HDIM)
    flat_index, key_mask = key_geometry(chosen_now, seq_start, blocks)
    near_keys = near_slabs(key_rows, seq_start, seq_first, length_local)
    near_values = near_slabs(value_rows, seq_start, seq_first, length_local)
    far_keys = far_rows(key_rows, flat_index)
    far_values = far_rows(value_rows, flat_index)
    near_scores = jnp.einsum(
        "bqnhe,btnhe->bnhqt", query_blocks, near_keys, preferred_element_type=jnp.float32
    )
    far_scores = jnp.einsum(
        "bqnhe,nhbke->bnhqk", query_blocks, far_keys, preferred_element_type=jnp.float32
    )
    scores = jnp.where(
        key_mask, HDIM ** (-0.5) * jnp.concatenate([near_scores, far_scores], -1), MASKED
    )
    return (query_blocks, near_keys, near_values, far_keys, far_values, flat_index, scores)


def attend(queries, key_rows, value_rows, chosen_now, seq_start, seq_first):
    query_blocks, near_keys, near_values, far_keys, far_values, flat_index, scores = (
        attention_setup(queries, key_rows, value_rows, chosen_now, seq_start, seq_first)
    )
    span = WIN + QB
    row_top = jnp.max(scores, -1, keepdims=True)
    exp_terms = jnp.exp(scores - row_top)
    row_total = jnp.sum(exp_terms, -1, keepdims=True)
    softmax_low = (exp_terms / row_total).astype(jnp.bfloat16)
    near_part = jnp.einsum(
        "bnhqt,btnhe->bqnhe",
        softmax_low[..., :span],
        near_values,
        preferred_element_type=jnp.float32,
    )
    far_part = jnp.einsum(
        "bnhqk,nhbke->bqnhe",
        softmax_low[..., span:],
        far_values,
        preferred_element_type=jnp.float32,
    )
    return ((near_part + far_part).reshape(queries.shape), row_top + jnp.log(row_total))


def spread_back(near_grad, far_grad, flat_index, seq_start, seq_first, total_rows):
    blocks, span, buckets, heads_local, head_size = near_grad.shape
    length_local = blocks * QB
    feature_width = heads_local * head_size
    segment = jnp.zeros((length_local + WIN, buckets, heads_local, head_size), jnp.float32)
    for offset_index in range(WIN // QB + 1):
        piece = near_grad[:, offset_index * QB : (offset_index + 1) * QB].reshape(
            length_local, buckets, heads_local, head_size
        )
        segment = segment.at[offset_index * QB : offset_index * QB + length_local].add(piece)
    full_rows = jnp.zeros((total_rows * buckets * heads_local, head_size), jnp.float32)
    full_rows = full_rows.at[flat_index.reshape(-1)].add(far_grad.reshape(-1, head_size))
    full_rows = full_rows.reshape(total_rows, buckets, feature_width)
    local_part = segment[WIN:].reshape(length_local, buckets, feature_width)
    earlier = jnp.where(seq_first, 0.0, segment[:WIN].reshape(WIN, buckets, feature_width))
    full_rows = lax.dynamic_update_slice_in_dim(
        full_rows,
        lax.dynamic_slice_in_dim(full_rows, seq_start, length_local, 0) + local_part,
        seq_start,
        0,
    )
    earlier_start = jnp.maximum(seq_start - WIN, 0)
    full_rows = lax.dynamic_update_slice_in_dim(
        full_rows,
        lax.dynamic_slice_in_dim(full_rows, earlier_start, WIN, 0) + earlier,
        earlier_start,
        0,
    )
    return full_rows


def attend_back(
    queries, key_rows, value_rows, chosen_now, seq_start, seq_first, log_total, grad_mixed
):
    query_blocks, near_keys, near_values, far_keys, far_values, flat_index, scores = (
        attention_setup(queries, key_rows, value_rows, chosen_now, seq_start, seq_first)
    )
    span = WIN + QB
    score_scale = HDIM ** (-0.5)
    grad_blocks = grad_mixed.reshape(query_blocks.shape)
    weights_full = jnp.exp(scores - log_total)
    softmax_low = weights_full.astype(jnp.bfloat16)
    grad_near_weights = jnp.einsum(
        "bqnhe,btnhe->bnhqt", grad_blocks, near_values, preferred_element_type=jnp.float32
    )
    grad_far_weights = jnp.einsum(
        "bqnhe,nhbke->bnhqk", grad_blocks, far_values, preferred_element_type=jnp.float32
    )
    grad_weights = jnp.concatenate([grad_near_weights, grad_far_weights], -1)
    row_dot = jnp.sum(weights_full * grad_weights, -1, keepdims=True)
    grad_scores = (weights_full * (grad_weights - row_dot)).astype(jnp.bfloat16)
    grad_near, grad_far = (grad_scores[..., :span], grad_scores[..., span:])
    grad_queries = score_scale * (
        jnp.einsum("bnhqt,btnhe->bqnhe", grad_near, near_keys, preferred_element_type=jnp.float32)
        + jnp.einsum("bnhqk,nhbke->bqnhe", grad_far, far_keys, preferred_element_type=jnp.float32)
    )
    near_key_grad = score_scale * jnp.einsum(
        "bnhqt,bqnhe->btnhe", grad_near, query_blocks, preferred_element_type=jnp.float32
    )
    far_key_grad = score_scale * jnp.einsum(
        "bnhqk,bqnhe->nhbke", grad_far, query_blocks, preferred_element_type=jnp.float32
    )
    near_value_grad = jnp.einsum(
        "bnhqt,bqnhe->btnhe",
        softmax_low[..., :span],
        grad_blocks,
        preferred_element_type=jnp.float32,
    )
    far_value_grad = jnp.einsum(
        "bnhqk,bqnhe->nhbke",
        softmax_low[..., span:],
        grad_blocks,
        preferred_element_type=jnp.float32,
    )
    total_rows = key_rows.shape[0]
    key_grad = spread_back(
        near_key_grad, far_key_grad, flat_index, seq_start, seq_first, total_rows
    )
    value_grad = spread_back(
        near_value_grad, far_value_grad, flat_index, seq_start, seq_first, total_rows
    )
    return (grad_queries.reshape(queries.shape), key_grad, value_grad)


def forward_pass(hidden, params, chosen_now, query_mask, seq_start, seq_first, finish):
    (
        ln1_gain,
        ln1_shift,
        w_qkv,
        b_qv,
        w_out,
        b_out,
        ln2_gain,
        ln2_shift,
        w_fc,
        b_fc,
        w_proj,
        b_proj,
    ) = params
    hidden_wide = hidden.astype(jnp.float32)
    normed_all = gather_rows(layer_norm(hidden_wide, ln1_gain, ln1_shift).astype(jnp.bfloat16))
    projected = jnp.einsum("pnd,jdc->jpnc", normed_all, w_qkv, preferred_element_type=jnp.float32)
    queries = (projected[0] + b_qv[0]).astype(jnp.bfloat16)
    key_rows, value_rows = (
        lax.all_gather(projected[1].astype(jnp.bfloat16), "seq", axis=0, tiled=True),
        lax.all_gather((projected[2] + b_qv[1]).astype(jnp.bfloat16), "seq", axis=0, tiled=True),
    )
    attended, log_total = attend(queries, key_rows, value_rows, chosen_now, seq_start, seq_first)
    mixed_rows = (attended * query_mask[:, :, None]).astype(jnp.bfloat16)
    middle = hidden_wide + scatter_product(mixed_rows, w_out, "pnc,cd->pnd") + b_out
    normed_mlp = gather_rows(layer_norm(middle, ln2_gain, ln2_shift).astype(jnp.bfloat16))
    pre_active = (
        jnp.einsum("pnd,df->pnf", normed_mlp, w_fc, preferred_element_type=jnp.float32) + b_fc
    )
    active = gelu_tanh(pre_active).astype(jnp.bfloat16)
    if not finish:
        return (
            normed_all,
            queries,
            key_rows,
            value_rows,
            log_total,
            mixed_rows,
            middle,
            normed_mlp,
            pre_active,
            active,
        )
    output = (middle + scatter_product(active, w_proj, "pnf,fd->pnd") + b_proj).astype(jnp.bfloat16)
    return (output, (key_rows, value_rows))


def backward_pass(hidden, upstream, params, chosen_now, query_mask, seq_start, seq_first):
    (
        ln1_gain,
        ln1_shift,
        w_qkv,
        b_qv,
        w_out,
        b_out,
        ln2_gain,
        ln2_shift,
        w_fc,
        b_fc,
        w_proj,
        b_proj,
    ) = params
    (
        normed_all,
        queries,
        key_rows,
        value_rows,
        log_total,
        mixed_rows,
        middle,
        normed_mlp,
        pre_active,
        active,
    ) = forward_pass(hidden, params, chosen_now, query_mask, seq_start, seq_first, False)
    upstream_all = gather_rows(upstream)
    grad_w_proj = jnp.einsum(
        "pnf,pnd->fd", active, upstream_all, preferred_element_type=jnp.float32
    )
    grad_b_proj = jnp.sum(upstream.astype(jnp.float32), axis=(0, 1))
    grad_active = jnp.einsum(
        "pnd,fd->pnf", upstream_all, w_proj, preferred_element_type=jnp.float32
    )
    unused_value, gelu_pull = jax.vjp(gelu_tanh, pre_active)
    grad_pre = gelu_pull(grad_active)[0].astype(jnp.bfloat16)
    grad_w_fc = jnp.einsum("pnd,pnf->df", normed_mlp, grad_pre, preferred_element_type=jnp.float32)
    grad_b_fc = jnp.sum(grad_pre.astype(jnp.float32), axis=(0, 1))
    grad_normed_mlp = scatter_product(grad_pre, w_fc, "pnf,df->pnd")
    unused_norm, second_pull = jax.vjp(layer_norm, middle, ln2_gain, ln2_shift)
    grad_mid_norm, grad_ln2_gain, grad_ln2_shift = second_pull(grad_normed_mlp)
    grad_middle = upstream.astype(jnp.float32) + grad_mid_norm
    grad_branch = grad_middle.astype(jnp.bfloat16)
    grad_b_out = jnp.sum(grad_branch.astype(jnp.float32), axis=(0, 1))
    branch_all = gather_rows(grad_branch)
    grad_w_out = jnp.einsum(
        "pnc,pnd->cd", mixed_rows, branch_all, preferred_element_type=jnp.float32
    )
    grad_mixed = jnp.einsum(
        "pnd,cd->pnc", branch_all, w_out, preferred_element_type=jnp.float32
    ).astype(jnp.bfloat16) * query_mask[:, :, None].astype(jnp.bfloat16)
    grad_queries, key_grad_all, value_grad_all = attend_back(
        queries, key_rows, value_rows, chosen_now, seq_start, seq_first, log_total, grad_mixed
    )
    key_grad, value_grad = (
        lax.psum_scatter(
            key_grad_all.astype(jnp.bfloat16), "seq", scatter_dimension=0, tiled=True
        ).astype(jnp.float32),
        lax.psum_scatter(
            value_grad_all.astype(jnp.bfloat16), "seq", scatter_dimension=0, tiled=True
        ).astype(jnp.float32),
    )
    grad_project = jnp.stack(
        [
            grad_queries.astype(jnp.bfloat16),
            key_grad.astype(jnp.bfloat16),
            value_grad.astype(jnp.bfloat16),
        ],
        2,
    )
    grad_w_qkv = jnp.einsum(
        "pnd,pnjc->jdc", normed_all, grad_project, preferred_element_type=jnp.float32
    )
    grad_b_qv = jnp.sum(grad_project[:, :, 0::2].astype(jnp.float32), axis=(0, 1))
    grad_normed = scatter_product(grad_project, w_qkv, "pnjc,jdc->pnd")
    unused_first, first_pull = jax.vjp(layer_norm, hidden.astype(jnp.float32), ln1_gain, ln1_shift)
    grad_in_norm, grad_ln1_gain, grad_ln1_shift = first_pull(grad_normed)
    grad_hidden = (grad_middle + grad_in_norm).astype(jnp.bfloat16)
    block_grads = (
        grad_ln1_gain,
        grad_ln1_shift,
        grad_w_qkv,
        grad_b_qv,
        grad_w_out,
        grad_b_out,
        grad_ln2_gain,
        grad_ln2_shift,
        grad_w_fc,
        grad_b_fc,
        grad_w_proj,
        grad_b_proj,
    )
    return (grad_hidden, block_grads)


def on_device(
    inputs,
    cotangent,
    lengths,
    chosen,
    ln1_gain,
    ln1_shift,
    w_qkv,
    b_qv,
    w_out,
    b_out,
    ln2_gain,
    ln2_shift,
    w_fc,
    b_fc,
    w_proj,
    b_proj,
):
    params = tuple(
        (
            weight_array[0]
            for weight_array in (
                ln1_gain,
                ln1_shift,
                w_qkv,
                b_qv,
                w_out,
                b_out,
                ln2_gain,
                ln2_shift,
                w_fc,
                b_fc,
                w_proj,
                b_proj,
            )
        )
    )
    section_index = lax.axis_index("section")
    section_count = lax.axis_size("section")
    seq_index = lax.axis_index("seq")
    tensor_index = lax.axis_index("tensor")
    tensor_count = lax.axis_size("tensor")
    micro_count, rows_local, buckets, feature_width = inputs.shape
    length_local = rows_local * tensor_count
    heads_width = w_qkv.shape[-1]
    seq_start = seq_index * length_local
    seq_first = seq_index == 0
    positions = seq_start + lax.broadcasted_iota(jnp.int32, (micro_count, length_local, buckets), 1)
    mask_all = (positions < lengths[:, None, :]).astype(jnp.float32)
    mask_rows = lax.dynamic_slice_in_dim(mask_all, tensor_index * rows_local, rows_local, 1)
    step_count = micro_count + section_count - 1
    chosen_section = chosen[0]
    received = jnp.zeros((rows_local, buckets, feature_width), jnp.bfloat16)
    stored = jnp.zeros((micro_count, rows_local, buckets, feature_width), jnp.bfloat16)
    outputs = jnp.zeros_like(stored)
    for step_index in range(step_count):
        micro_index = step_index - section_index
        running = (micro_index >= 0) & (micro_index < micro_count)
        slot_index = jnp.clip(micro_index, 0, micro_count - 1)
        block_in = jnp.where(
            section_index == 0, lax.dynamic_index_in_dim(inputs, slot_index, 0, False), received
        )
        chosen_now = lax.dynamic_index_in_dim(chosen_section, slot_index, 0, False)
        query_mask = lax.dynamic_index_in_dim(mask_all, slot_index, 0, False)
        result, key_pair = forward_pass(
            block_in, params, chosen_now, query_mask, seq_start, seq_first, True
        )
        stored = jnp.where(
            running, lax.dynamic_update_index_in_dim(stored, block_in, slot_index, 0), stored
        )
        outputs = jnp.where(
            running, lax.dynamic_update_index_in_dim(outputs, result, slot_index, 0), outputs
        )
        received = from_behind(result, "section", 1)
    back_received = jnp.zeros((rows_local, buckets, feature_width), jnp.bfloat16)
    in_grads = jnp.zeros_like(stored)
    totals = None
    for step_index in range(step_count):
        micro_index = step_index - (section_count - 1 - section_index)
        running = (micro_index >= 0) & (micro_index < micro_count)
        slot_index = jnp.clip(micro_index, 0, micro_count - 1)
        chosen_now = lax.dynamic_index_in_dim(chosen_section, slot_index, 0, False)
        query_mask = lax.dynamic_index_in_dim(mask_all, slot_index, 0, False)
        local_mask = lax.dynamic_index_in_dim(mask_rows, slot_index, 0, False)
        top_grad = (
            lax.dynamic_index_in_dim(cotangent, slot_index, 0, False).astype(jnp.float32)
            * local_mask[:, :, None]
        ).astype(jnp.bfloat16)
        upstream = jnp.where(section_index == section_count - 1, top_grad, back_received)
        hidden = lax.dynamic_index_in_dim(stored, slot_index, 0, False)
        grad_hidden, block_grads = backward_pass(
            hidden, upstream, params, chosen_now, query_mask, seq_start, seq_first
        )
        block_grads = tuple(
            (jnp.where(running, grad_part, jnp.zeros_like(grad_part)) for grad_part in block_grads)
        )
        totals = (
            block_grads
            if step_index == 0
            else tuple(
                (total_part + grad_part for total_part, grad_part in zip(totals, block_grads))
            )
        )
        in_grads = jnp.where(
            running, lax.dynamic_update_index_in_dim(in_grads, grad_hidden, slot_index, 0), in_grads
        )
        back_received = from_behind(grad_hidden, "section", -1)
    (
        sum_ln1_gain,
        sum_ln1_shift,
        sum_w_qkv,
        sum_b_qv,
        sum_w_out,
        sum_b_out,
        sum_ln2_gain,
        sum_ln2_shift,
        sum_w_fc,
        sum_b_fc,
        sum_w_proj,
        sum_b_proj,
    ) = totals
    part_qkv, part_out, part_fc, part_proj = (
        lax.psum_scatter(
            sum_w_qkv.astype(jnp.bfloat16), "seq", scatter_dimension=1, tiled=True
        ).astype(jnp.float32),
        lax.psum_scatter(
            sum_w_out.astype(jnp.bfloat16), "seq", scatter_dimension=1, tiled=True
        ).astype(jnp.float32),
        lax.psum_scatter(
            sum_w_fc.astype(jnp.bfloat16), "seq", scatter_dimension=0, tiled=True
        ).astype(jnp.float32),
        lax.psum_scatter(
            sum_w_proj.astype(jnp.bfloat16), "seq", scatter_dimension=1, tiled=True
        ).astype(jnp.float32),
    )
    bias_qv = lax.dynamic_update_slice_in_dim(
        jnp.zeros((2, feature_width), jnp.float32), sum_b_qv, tensor_index * heads_width, 1
    )
    units_local = sum_b_fc.shape[0]
    bias_fc = lax.dynamic_update_slice_in_dim(
        jnp.zeros((units_local * tensor_count,), jnp.float32),
        sum_b_fc,
        tensor_index * units_local,
        0,
    )
    small_sums = lax.psum(
        (
            sum_ln1_gain,
            sum_ln1_shift,
            bias_qv,
            sum_b_out,
            sum_ln2_gain,
            sum_ln2_shift,
            bias_fc,
            sum_b_proj,
        ),
        ("seq", "tensor"),
    )
    return (
        outputs[None],
        in_grads[None],
        small_sums[0][None],
        small_sums[1][None],
        part_qkv[None],
        small_sums[2][None],
        part_out[None],
        small_sums[3][None],
        small_sums[4][None],
        small_sums[5][None],
        part_fc[None],
        small_sums[6][None],
        part_proj[None],
        small_sums[7][None],
    )


STREAMS = 2
NRM, NMLP, UPS, BRN, ACT, GPRE, MIX, DQKV = range(8)
F32 = jnp.float32
LOW = jnp.bfloat16
MESH_ID = pl.DeviceIdType.MESH


def dot_nn(left, right):
    return lax.dot_general(left, right, (((1,), (0,)), ((), ())), preferred_element_type=F32)


def dot_nt(left, right):
    return lax.dot_general(left, right, (((1,), (1,)), ((), ())), preferred_element_type=F32)


def dot_tn(left, right):
    return lax.dot_general(left, right, (((0,), (0,)), ((), ())), preferred_element_type=F32)


def standard(rows):
    centred = rows - jnp.mean(rows, axis=-1, keepdims=True)
    scale = lax.rsqrt(jnp.mean(centred * centred, axis=-1, keepdims=True) + NORM_EPS)
    return centred * scale, scale


def standard_back(grad, xhat, scale):
    inner = jnp.mean(grad * xhat, axis=-1, keepdims=True)
    return scale * (grad - jnp.mean(grad, axis=-1, keepdims=True) - xhat * inner)


def column_sum(rows):
    return jnp.sum(rows.astype(F32), axis=0, keepdims=True)


def relay_kernel(names, *refs):
    r = types.SimpleNamespace(**dict(zip(names, refs)))
    a, c, t = (lax.axis_index(name) for name in ("section", "seq", "tensor"))
    lines = lax.axis_size("section")
    chips = lax.axis_size("tensor")
    rows, buckets, width = r.inputs.shape[1:]
    half_width = width // 2
    local = rows * chips
    total = 2 * local
    stream_rows = local // STREAMS
    head_width = r.wo_in.shape[0]
    heads = head_width // HDIM
    blocks = local // QB
    units = r.wp_in.shape[0]
    scale = HDIM ** (-0.5)
    streams = range(STREAMS)

    def remote(src, dst, send, recv, **target):
        return pltpu.make_async_remote_copy(
            src_ref=src,
            dst_ref=dst,
            send_sem=send,
            recv_sem=recv,
            device_id=target,
            device_id_type=MESH_ID,
        )

    def drain(ref, sem):
        pltpu.make_async_copy(ref, ref, sem).wait()

    def row_block(index, size):
        return pl.ds(pl.multiple_of(index * size, size), size)

    near_chip = t + 1 - 2 * (t % 2)
    over_chip = (t + 2) % 4
    across_chip = 3 - t
    middle_chip = (t == 1) | (t == 2)
    end_chip = (t == 0) | (t == 3)
    owned = stream_rows // 2
    mine = row_block(t - 1, owned)
    my_half = row_block(c, local)

    r.kv[...] = jnp.zeros(r.kv.shape, LOW)

    barrier = pltpu.get_barrier_semaphore()
    greeted = 0
    for line in range(lines):
        for chip in range(chips):
            for core in range(2):
                if (line, chip, core) != (0, 0, 0) and (core == 0 or line * chip == 0):
                    there = {
                        "section": (a + line) % lines,
                        "seq": (c + core) % 2,
                        "tensor": (t + chip) % chips,
                    }
                    pl.semaphore_signal(barrier, inc=1, device_id=there, device_id_type=MESH_ID)
                    greeted += 1
    pl.semaphore_wait(barrier, greeted)

    def beside(s):
        return s + 1 - 2 * (s % 2)

    def above(s):
        return (s + 2) % 4

    def store(p):
        return (r.wq, r.wo, r.wf, r.wp)[p]

    def source(p):
        return (r.wq_in, r.wo_in, r.wf_in, r.wp_in)[p]

    def height(p):
        return source(p).shape[0]

    def core_half(p, s, core):
        return store(p).at[s, row_block(core, height(p) // 2)]

    def first_hop(p, s, neighbour, which):
        return remote(
            source(p).at[row_block(c, height(p) // 2)],
            core_half(p, s, c),
            r.w_first_s.at[p, which],
            r.w_first_r.at[s, p],
            section=neighbour,
        )

    def second_hop(p, s, which):
        view = store(p).at[s, row_block(2 * c + which, height(p) // 4)]
        return remote(
            view, view, r.w_second_s.at[s, p], r.w_second_r.at[s, p, which], section=3 - s
        )

    def core_hop(p, s, core):
        view = core_half(p, s, core)
        return remote(view, view, r.w_core_s.at[s, p], r.w_core_r.at[s, p], seq=1 - c)

    def own_copy(p):
        return pltpu.make_async_copy(source(p), store(p).at[a], r.w_own.at[p])

    def pass_on(s, p, which):
        line = (beside(s), above(s))[which]

        @pl.when(a == line)
        def _():
            first_hop(p, s, line, which).wait_recv()
            second_hop(p, s, which).start()
            core_hop(p, s, c).start()

    def pass_all(s, pieces):
        for p in pieces:
            for which in range(2):
                pass_on(s, p, which)

    def pass_far(s, p):
        @pl.when(a == 3 - s)
        def _():
            second_hop(p, s, 0).wait_recv()
            second_hop(p, s, 1).wait_recv()
            core_hop(p, s, c).start()

    def need(s, p):
        @pl.when(s == 0)
        def _():
            if p < 2:
                pass_all(0, (p,))
            pass_far(0, p)

        @pl.when(a == s)
        def _():
            own_copy(p).wait()

        @pl.when(a != s)
        def _():
            core_hop(p, s, 1 - c).wait_recv()

    def small_copy(step, line, slot):
        return remote(
            r.small_own, r.small.at[slot], r.small_s.at[step], r.small_r.at[slot], section=line
        )

    def count_copy(step, line, slot):
        return remote(
            r.count_own.at[line],
            r.count.at[slot],
            r.count_s.at[step],
            r.count_r.at[slot],
            section=line,
        )

    singles = (r.ln1_gain, r.ln1_shift, r.ln2_gain, r.ln2_shift, r.b_out, r.b_proj)
    for place, single in enumerate(singles):
        r.small_own[place : place + 1] = single[...]
    r.small_own[6:7, :units] = r.b_fc[...]
    r.small_own[7:8, :head_width] = r.b_qv[0:1]
    r.small_own[7:8, half_width : half_width + head_width] = r.b_qv[1:2]
    for step in range(1, lines):
        small_copy(step - 1, (a + step) % lines, a).start()
    for p in range(4):
        for which, line in enumerate((beside(a), above(a))):
            first_hop(p, a, line, which).start()
    for p in range(4):
        own_copy(p).start()
    r.small[a] = r.small_own[...]

    def iota(shape, dimension):
        return lax.broadcasted_iota(jnp.int32, shape, dimension)

    square = jnp.where(iota((KSEL, KSEL), 0) == iota((KSEL, KSEL), 1), 1.0, 0.0).astype(LOW)
    position = iota((KSEL, total), 1).astype(F32)
    for pair in range(lines * heads):
        line, head = pair // heads, pair % heads
        columns = dot_nt(square, r.chosen[pair].astype(F32).astype(LOW))
        for block in range(blocks):
            pick = head * blocks + block
            r.count_own[line, pick : pick + 1, :] = jnp.sum(
                jnp.where(columns[:, block : block + 1] == position, 1.0, 0.0),
                axis=0,
                keepdims=True,
            )
    for step in range(1, lines):
        count_copy(step - 1, (a + step) % lines, a).start()
    r.count[a] = r.count_own[a]

    NEAR, OVER, ACROSS = range(3)

    def gather(buffer, s, kind, j, owner, target, slot):
        view = buffer.at[s, j, row_block(owner - 1, owned)]
        return remote(
            view, view, r.ag_s.at[kind, j, slot], r.ag_r.at[kind, j, slot], tensor=target
        )

    def used_before(s, kind):
        return s > 0 if kind < 2 else s < lines - 1

    def gather_start(buffer, s, kind, j):
        @pl.when(used_before(s, kind))
        def _():
            gather_sent(buffer, s, kind, j)

        gather(buffer, s, kind, j, t, over_chip, OVER).start()
        gather(buffer, s, kind, j, t, across_chip, ACROSS).start()
        gather(buffer, s, kind, j, t, near_chip, NEAR).start()

    def gather_wait(buffer, s, kind, j):
        @pl.when(middle_chip)
        def _():
            gather(buffer, s, kind, j, across_chip, across_chip, ACROSS).wait_recv()

        @pl.when(end_chip)
        def _():
            gather(buffer, s, kind, j, near_chip, near_chip, NEAR).wait_recv()
            gather(buffer, s, kind, j, over_chip, over_chip, OVER).wait_recv()

    def gather_sent(buffer, s, kind, j):
        gather(buffer, s, kind, j, t, over_chip, OVER).wait_send()
        gather(buffer, s, kind, j, t, across_chip, ACROSS).wait_send()
        gather(buffer, s, kind, j, t, near_chip, NEAR).wait_send()

    def scatter(s, kind, j, owner, slot):
        return remote(
            r.part.at[kind, j, row_block(owner - 1, owned)],
            r.arrived.at[s, kind, j, slot],
            r.rs_s.at[kind, j, slot],
            r.rs_r.at[kind, j, slot],
            tensor=owner,
        )

    def scatter_start(s, kind, j, product):
        @pl.when(used_before(s, kind))
        def _():
            scatter_sent(s, kind, j)

        r.part[kind, j] = product.astype(LOW)

        @pl.when(end_chip)
        def _():
            scatter(s, kind, j, over_chip, OVER).start()
            scatter(s, kind, j, near_chip, NEAR).start()

        @pl.when(middle_chip)
        def _():
            scatter(s, kind, j, across_chip, ACROSS).start()

    def scatter_sum(s, kind, j):
        result = r.part[kind, j, mine].astype(F32)
        for slot in (NEAR, ACROSS, OVER):
            scatter(s, kind, j, t, slot).wait_recv()
            result = result + r.arrived[s, kind, j, slot].astype(F32)
        return result

    def scatter_sent(s, kind, j):
        @pl.when(end_chip)
        def _():
            scatter(s, kind, j, over_chip, OVER).wait_send()
            scatter(s, kind, j, near_chip, NEAR).wait_send()

        @pl.when(middle_chip)
        def _():
            scatter(s, kind, j, across_chip, ACROSS).wait_send()

    own_rows = (r.nrm, r.nmlp, r.ups, r.brn, r.act, r.gpre, r.mix, r.dqkv)
    all_rows = (
        r.all_nrm,
        r.all_nmlp,
        r.all_ups,
        r.all_brn,
        r.all_act,
        r.all_gpre,
        r.all_mix,
        r.all_dqkv,
    )

    def rows_copy(index, s, same, stays=False):
        core = c if same else 1 - c
        src = own_rows[index].at[s]
        dst = all_rows[index].at[a, c]
        if index <= BRN:
            src = src.at[:, :, row_block(core, half_width)]
        recv = r.heads_r.at[a] if index == DQKV else r.rows_r.at[index]
        if stays:
            return pltpu.make_async_copy(src, dst, recv)
        if same:
            return remote(src, dst, r.rows_s.at[index, s, 0], recv, section=s)
        return remote(src, dst, r.rows_s.at[index, s, 1], recv, section=s, seq=1 - c)

    passed_rows = {UPS: r.pass_ups, GPRE: r.pass_gpre}
    places = {UPS: 0, GPRE: 1}

    def detour_copy(index):
        return remote(
            own_rows[index].at[0],
            passed_rows[index],
            r.pass_s.at[places[index]],
            r.pass_r.at[places[index]],
            section=1,
        )

    def passed_copies(index):
        copies = []
        for step in range(2 if index <= BRN else 1):
            core = (c + step) % 2
            src = passed_rows[index]
            if index <= BRN:
                src = src.at[:, :, row_block(core, half_width)]
            send = r.pass_on_s.at[places[index], step]
            dst = all_rows[index].at[3, c]
            copies.append(remote(src, dst, send, r.rows_r.at[index], section=0, seq=core))
        return copies

    def pass_rows(index):
        @pl.when(a == 1)
        def _():
            detour_copy(index).wait_recv()
            for copy in passed_copies(index):
                copy.start()

    def goes_direct(index, s):
        return jnp.logical_not((a == 3) & (s == 0)) if index in passed_rows else a >= 0

    def rows_start(index, s):
        if index in passed_rows:

            @pl.when((a == 3) & (s == 0))
            def _():
                detour_copy(index).start()

        @pl.when(a == s)
        def _():
            rows_copy(index, s, True, True).start()

        @pl.when((a != s) & goes_direct(index, s))
        def _():
            rows_copy(index, s, True).start()

        if index <= BRN:

            @pl.when(goes_direct(index, s))
            def _():
                rows_copy(index, s, False).start()

    def forward_rows(s):
        for index in (NRM, MIX, NMLP, ACT):
            rows_start(index, s)

    def rows_sent(index, s):
        @pl.when((a != s) & goes_direct(index, s))
        def _():
            rows_copy(index, s, True).wait_send()

        if index <= BRN:

            @pl.when(goes_direct(index, s))
            def _():
                rows_copy(index, s, False).wait_send()

    def share_copy(index, core):
        view = all_rows[index].at[:, core]
        return remote(view, view, r.share_s.at[index - ACT], r.share_r.at[index - ACT], seq=1 - c)

    def share_heads(line, core):
        view = r.all_dqkv.at[line, core]
        return remote(view, view, r.heads_s.at[line], r.heads_sr.at[line], seq=1 - c)

    def share(index):
        drain(all_rows[index].at[:, c], r.rows_r.at[index])
        share_copy(index, c).start()

    def norm_copy(s):
        return remote(
            r.norm_part.at[s], r.norm_all.at[a], r.norm_s.at[s], r.norm_r, section=s
        )

    def norm_start(s):
        @pl.when(a == s)
        def _():
            pltpu.make_async_copy(r.norm_part.at[s], r.norm_all.at[a], r.norm_r).start()

        @pl.when(a != s)
        def _():
            norm_copy(s).start()

    def home_copy(what, s, j):
        src, dst, send, recv = what
        chip = 2 * j + t - 1
        return remote(src.at[s, j], dst.at[a], send.at[s, j], recv, section=s, tensor=chip)

    def home_start(what, s):
        @pl.when(middle_chip)
        def _():
            for j in streams:
                home_copy(what, s, j).start()

    def home_sent(what, s):
        @pl.when(middle_chip)
        def _():
            for j in streams:
                home_copy(what, s, j).wait_send()

    out_home = (r.out_low, r.acts, r.out_s, r.out_r)
    grad_home = (r.grad_low, r.grads, r.grad_s, r.grad_r)

    length = r.lengths[a // buckets, a % buckets]
    key = iota((stream_rows, total), 1)
    for j in streams:
        query = c * local + j * stream_rows + iota((stream_rows, total), 0)
        r.near[j] = jnp.where((query >= key) & (query - key < WIN), 1.0, 0.0)
    key_row = iota((1, total), 1)

    def row_mask(place):
        return jnp.where(place < length, 1.0, 0.0)

    def stream_mask(j):
        return row_mask(c * local + j * stream_rows + iota((stream_rows, 1), 0))

    def multiplicity(s, j, head):
        block = j * stream_rows // QB
        pick = head * blocks + block
        limit = (c * blocks + block) * QB - WIN
        return r.near[j] + jnp.where(key_row <= limit, r.count[s, pick : pick + 1, :], 0.0)

    def head_cols(head):
        return slice(head * HDIM, (head + 1) * HDIM)

    def kv_copy(s, j):
        view = r.kv.at[s, :, j * stream_rows : (j + 1) * stream_rows]
        return remote(view, view, r.kv_s.at[s, j], r.kv_r.at[s, j], seq=1 - c)

    def dkv_copy(s):
        return remote(r.dkv_out.at[s], r.dkv_in.at[s], r.dkv_s.at[s], r.dkv_r.at[s], seq=1 - c)

    def own_sequence(ref):
        both = ref[a // buckets].astype(F32)
        picked = both[:, 0, :]
        for bucket in range(1, buckets):
            picked = jnp.where(a % buckets == bucket, both[:, bucket, :], picked)
        return picked

    def first_copy(stream):
        return remote(
            r.first_out, r.first_in.at[stream], r.first_s, r.first_r.at[stream], tensor=1 + t % 2
        )

    own_place = c * local + t * rows + iota((rows, 1), 0)
    r.first_out[0] = own_sequence(r.inputs).astype(LOW)
    r.first_out[1] = (own_sequence(r.cotangent) * row_mask(own_place)).astype(LOW)
    first_copy(t // 2).start()
    r.norm_part[...] = jnp.zeros_like(r.norm_part)

    def first_rows(j):
        @pl.when(middle_chip)
        def _():
            first_copy(j).wait_recv()
            r.hidden[j] = r.first_in[j, 0].astype(F32)
            r.upstream[j] = r.first_in[j, 1]

    def on_owner(stage):
        def run(s, j):
            @pl.when(middle_chip)
            def _():
                stage(s, j)

        return run

    @on_owner
    def enter(s, j):
        xhat, inverse = standard(r.hidden[j])
        r.xhat1[s, j] = xhat
        r.inv1[s, j] = jnp.broadcast_to(inverse, (owned, 128))
        r.nrm[s, j, mine] = (xhat * r.small[s, 0:1] + r.small[s, 1:2]).astype(LOW)
        gather_start(r.nrm, s, 0, j)

    def project(s, j):
        gather_wait(r.nrm, s, 0, j)
        normed = r.nrm[s, j]
        place = row_block(c * STREAMS + j, stream_rows)
        bias_v = r.small[s, 7:8, half_width : half_width + head_width]
        key_rows = dot_nt(normed, r.wq[s, head_width : 2 * head_width])
        value_rows = dot_nt(normed, r.wq[s, 2 * head_width : 3 * head_width]) + bias_v
        r.kv[s, 0, place] = key_rows.astype(LOW)
        r.kv[s, 1, place] = value_rows.astype(LOW)

    def ask(s, j):
        queries = dot_nt(r.nrm[s, j], r.wq[s, 0:head_width]) + r.small[s, 7:8, :head_width]
        r.qry[s, j] = queries.astype(LOW)

    def attend_line(s, j):
        mixed = []
        for head in range(heads):
            cols = head_cols(head)
            times = multiplicity(s, j, head)
            scores = scale * dot_nt(r.qry[s, j, :, cols], r.kv[s, 0, :, cols])
            scores = jnp.where(times > 0.0, scores, MASKED)
            top = jnp.max(scores, axis=-1, keepdims=True)
            terms = times * jnp.exp(scores - top)
            weights = terms / jnp.sum(terms, axis=-1, keepdims=True)
            r.soft[s, j, head] = weights
            mixed.append(dot_nn(weights.astype(LOW), r.kv[s, 1, :, cols]))
        r.mix[s, j] = (jnp.concatenate(mixed, axis=-1) * stream_mask(j)).astype(LOW)

    def leave_attention(s, j):
        scatter_start(s, 0, j, dot_nn(r.mix[s, j], r.wo[s]))

    @on_owner
    def between(s, j):
        middle = r.hidden[j] + scatter_sum(s, 0, j) + r.small[s, 4:5]
        r.middle[j] = middle
        xhat, inverse = standard(middle)
        r.xhat2[s, j] = xhat
        r.inv2[s, j] = jnp.broadcast_to(inverse, (owned, 128))
        r.nmlp[s, j, mine] = (xhat * r.small[s, 2:3] + r.small[s, 3:4]).astype(LOW)
        gather_start(r.nmlp, s, 1, j)

    def feed(s, j):
        gather_wait(r.nmlp, s, 1, j)
        before = dot_nn(r.nmlp[s, j], r.wf[s]) + r.small[s, 6:7, :units]
        bend = jnp.tanh(0.7978845608028654 * (before + 0.044715 * before * before * before))
        r.act[s, j] = (0.5 * before * (1.0 + bend)).astype(LOW)
        r.slope[s, j] = 0.5 * (1.0 + bend) + 0.5 * before * (1.0 - bend * bend) * (
            0.7978845608028654 * (1.0 + 3 * 0.044715 * before * before)
        )


    def leave_feed(s, j):
        scatter_start(s, 1, j, dot_nn(r.act[s, j], r.wp[s]))

    @on_owner
    def finish(s, j):
        result = r.middle[j] + scatter_sum(s, 1, j) + r.small[s, 5:6]
        r.out_low[s, j] = result.astype(LOW)
        r.hidden[j] = result.astype(LOW).astype(F32)

    def small_ready(s):
        @pl.when(a != s)
        def _():
            small_copy(0, a, s).wait_recv()

    small_ready(0)
    for j in streams:
        first_rows(j)
        enter(0, j)

    def forward(s, _):
        need(s, 0)
        need(s, 1)

        @pl.when(a != s)
        def _():
            count_copy(0, a, s).wait_recv()

        for j in streams:
            project(s, j)

            @pl.when(c == 0)
            def _():
                kv_copy(s, j).start()

            ask(s, j)
            if j == 0:

                @pl.when(c == 1)
                def _():
                    for other in streams:
                        kv_copy(s, other).wait_recv()

            if j == STREAMS - 1:

                @pl.when(s == 0)
                def _():
                    pass_all(0, (2,))

            attend_line(s, j)
            leave_attention(s, j)

        @pl.when(s == 0)
        def _():
            pass_all(0, (3,))
            for later in range(1, lines):
                pass_all(later, (0, 1, 2))

        @pl.when(s == 1)
        def _():
            pass_far(1, 2)
            pass_far(1, 3)
            for later in range(2, lines):
                for p in range(4):
                    pass_far(later, p)

        for j in streams:
            between(s, j)
        @pl.when(s == 0)
        def _():
            for later in range(1, lines):
                pass_all(later, (3,))

        need(s, 2)
        for j in streams:
            feed(s, j)
            if j == 0:
                need(s, 3)
            leave_feed(s, j)


        @pl.when(s >= 2)
        def _():
            forward_rows(s - 2)


        @pl.when(s + 1 < lines)
        def _():
            small_ready(s + 1)

        for j in streams:
            finish(s, j)

            @pl.when(s + 1 < lines)
            def _():
                enter(s + 1, j)

        home_start(out_home, s)

        @pl.when(s == 0)
        def _():
            pass_far(1, 0)
            pass_far(1, 1)

        return 0

    lax.fori_loop(0, lines, forward, 0)

    @on_owner
    def turn(s, j):
        upstream = r.upstream[j]
        r.ups[s, j, mine] = upstream
        gather_start(r.ups, s, 2, j)
        r.norm_part[s, 5:6] += column_sum(upstream)

    def feed_back(s, j):
        gather_wait(r.ups, s, 2, j)
        grad_pre = (dot_nt(r.ups[s, j], r.wp[s]) * r.slope[s, j]).astype(LOW)
        r.gpre[s, j] = grad_pre
        scatter_start(s, 2, j, dot_nt(grad_pre, r.wf[s]))
        r.norm_part[s, 6:7, :units] += column_sum(grad_pre)

    @on_owner
    def between_back(s, j):
        grad = scatter_sum(s, 2, j)
        xhat = r.xhat2[s, j]
        upstream = r.upstream[j].astype(F32)
        grad_middle = upstream + standard_back(
            grad * r.small[s, 2:3], xhat, r.inv2[s, j, :, 0:1]
        )
        r.middle[j] = grad_middle
        branch = grad_middle.astype(LOW)
        r.brn[s, j, mine] = branch
        gather_start(r.brn, s, 3, j)
        r.norm_part[s, 2:3] += column_sum(grad * xhat)
        r.norm_part[s, 3:4] += column_sum(grad)
        r.norm_part[s, 4:5] += column_sum(branch)

    def mixed_back(s, j):
        gather_wait(r.brn, s, 3, j)
        r.gmix[j] = (dot_nt(r.brn[s, j], r.wo[s]) * stream_mask(j)).astype(LOW)

    def attend_line_back(s, j):
        grad_q, grad_k, grad_v = [], [], []
        for head in range(heads):
            cols = head_cols(head)
            weights = r.soft[s, j, head]
            grad_head = r.gmix[j, :, cols]
            grad_weights = dot_nt(grad_head, r.kv[s, 1, :, cols])
            inner = jnp.sum(weights * grad_weights, axis=-1, keepdims=True)
            grad_scores = (weights * (grad_weights - inner)).astype(LOW)
            grad_k.append(scale * dot_tn(grad_scores, r.qry[s, j, :, cols]))
            grad_v.append(dot_tn(weights.astype(LOW), grad_head))
            grad_q.append(scale * dot_nn(grad_scores, r.kv[s, 0, :, cols]))
        for which, grad in enumerate((grad_k, grad_v)):
            grad = jnp.concatenate(grad, axis=-1)
            r.dkv_all[which] = grad if j == STREAMS - 1 else r.dkv_all[which] + grad
        grad_q = jnp.concatenate(grad_q, axis=-1).astype(LOW)
        r.dqkv[s, 0, j] = grad_q
        r.norm_part[s, 7:8, :head_width] += column_sum(grad_q)

    def join_keys(s, j):
        for which in range(2):
            joined = r.dkv_all[which, row_block(c * STREAMS + j, stream_rows)].astype(LOW)
            r.dqkv[s, 1 + which, j] = joined
            if which == 1:
                lanes = slice(half_width, half_width + head_width)
                r.norm_part[s, 7:8, lanes] += column_sum(joined)

    def leave_back(s, j):
        product = dot_nn(r.dqkv[s, 0, j], r.wq[s, 0:head_width])
        for which in range(1, 3):
            weight = r.wq[s, which * head_width : (which + 1) * head_width]
            product = product + dot_nn(r.dqkv[s, which, j], weight)
        scatter_start(s, 3, j, product)

    @on_owner
    def finish_back(s, j):
        grad = scatter_sum(s, 3, j)
        xhat = r.xhat1[s, j]
        result = r.middle[j] + standard_back(
            grad * r.small[s, 0:1], xhat, r.inv1[s, j, :, 0:1]
        )
        r.upstream[j] = result.astype(LOW)
        r.grad_low[s, j] = result.astype(LOW)
        r.norm_part[s, 0:1] += column_sum(grad * xhat)
        r.norm_part[s, 1:2] += column_sum(grad)

    last_first = tuple(reversed(streams))
    for j in last_first:
        turn(lines - 1, j)

    def backward(index, _):
        s = lines - 1 - index
        for j in last_first:
            feed_back(s, j)
        rows_start(UPS, s)
        rows_start(GPRE, s)

        @pl.when(index < 2)
        def _():
            forward_rows(lines - 2 + index)

        @pl.when(index == lines - 2)
        def _():
            share(ACT)
            share(MIX)

        for j in last_first:
            between_back(s, j)
        for j in last_first:
            mixed_back(s, j)
            if j == 0:
                rows_start(BRN, s)
            attend_line_back(s, j)

            @pl.when(c == 1)
            def _():
                join_keys(s, j)
                leave_back(s, j)

        @pl.when(c == 1)
        def _():
            r.dkv_out[s] = r.dkv_all[:, 0:local].astype(LOW)
            dkv_copy(s).start()

        @pl.when(c == 0)
        def _():
            dkv_copy(s).wait_recv()
            r.dkv_all[:, 0:local] += r.dkv_in[s].astype(F32)
            for j in last_first:
                join_keys(s, j)
                leave_back(s, j)

        rows_start(DQKV, s)

        @pl.when(s == 0)
        def _():
            pass_rows(UPS)
            pass_rows(GPRE)

        for j in last_first:
            finish_back(s, j)

            @pl.when(s > 0)
            def _():
                turn(s - 1, j)

        norm_start(s)
        home_start(grad_home, s)
        return 0

    lax.fori_loop(0, lines, backward, 0)

    share(GPRE)

    drain(r.norm_all, r.norm_r)
    slot = c * chips + t
    norm_sum = r.norm_all[0]
    for line in range(1, lines):
        norm_sum = norm_sum + r.norm_all[line]
    r.ends[slot] = norm_sum

    def ends_copy(step):
        core, chip = step // chips, step % chips
        view = r.ends.at[slot]
        return remote(
            view,
            view,
            r.ends_s.at[step - 1],
            r.ends_r,
            seq=(c + core) % 2,
            tensor=(t + chip) % chips,
        )

    for step in range(1, 2 * chips):
        ends_copy(step).start()

    for line in range(lines):
        drain(r.all_dqkv.at[line, c], r.heads_r.at[line])
        share_heads(line, c).start()

    for index in (UPS, GPRE):

        @pl.when(a == 3)
        def _():
            detour_copy(index).wait_send()

        @pl.when(a == 1)
        def _():
            for copy in passed_copies(index):
                copy.wait_send()

    for kind, buffer in enumerate((r.nrm, r.nmlp, r.ups, r.brn)):
        for j in streams:
            scatter_sent(0, kind, j)

            @pl.when(middle_chip)
            def _():
                gather_sent(buffer, 0, kind, j)

    for index in range(ACT):
        drain(all_rows[index], r.rows_r.at[index])
    for index in range(ACT, DQKV):
        share_copy(index, 1 - c).wait_recv()
        share_copy(index, c).wait_send()
    for line in range(lines):
        share_heads(line, 1 - c).wait_recv()
        share_heads(line, c).wait_send()
    drain(r.acts, r.out_r)
    drain(r.grads, r.grad_r)
    drain(r.ends.at[0 : 2 * chips - 1], r.ends_r)
    for step in range(1, 2 * chips):
        ends_copy(step).wait_send()
    for step in range(1, lines):
        small_copy(step - 1, (a + step) % lines, a).wait_send()
        count_copy(step - 1, (a + step) % lines, a).wait_send()
    for p in range(4):
        for which, line in enumerate((beside(a), above(a))):
            first_hop(p, a, line, which).wait_send()

    first_copy(t // 2).wait_send()

    def sent(s, _):
        home_sent(out_home, s)
        home_sent(grad_home, s)

        @pl.when(a != s)
        def _():
            norm_copy(s).wait_send()

        @pl.when(c == 0)
        def _():
            for j in streams:
                kv_copy(s, j).wait_send()

        @pl.when(c == 1)
        def _():
            dkv_copy(s).wait_send()

        for index in range(8):
            rows_sent(index, s)
        for p in range(4):

            @pl.when((a == beside(s)) | (a == above(s)))
            def _():
                second_hop(p, s, 0).wait_send()

            @pl.when(a != s)
            def _():
                core_hop(p, s, c).wait_send()

        return 0

    lax.fori_loop(0, lines, sent, 0)


def relay_call(inputs, cotangent, lengths, chosen, singles, weights):
    lines = lax.axis_size("section")
    chips = lax.axis_size("tensor")
    rows, buckets, width = inputs.shape[1:]
    local, total, half = rows * chips, 2 * rows * chips, width // 2
    head_width, units = weights["wo_in"].shape[0], weights["wp_in"].shape[0]
    heads = head_width // HDIM
    stream = local // STREAMS
    peers, owned = chips - 1, stream // 2
    vmem, dma = pltpu.VMEM, pltpu.SemaphoreType.DMA
    operands = dict(
        inputs=inputs,
        cotangent=cotangent,
        lengths=lengths,
        chosen=chosen,
        **singles,
        **weights,
    )

    def space(name):
        if name in weights:
            return pl.ANY
        return pltpu.SMEM if operands[name] is lengths else pltpu.VMEM

    sums = dict(
        acts=((lines, rows, width), LOW),
        grads=((lines, rows, width), LOW),
        ends=((2 * chips, 8, width), F32),
    )
    gathered = dict(
        all_nrm=((lines, 2, STREAMS, stream, half), LOW),
        all_nmlp=((lines, 2, STREAMS, stream, half), LOW),
        all_ups=((lines, 2, STREAMS, stream, half), LOW),
        all_brn=((lines, 2, STREAMS, stream, half), LOW),
        all_act=((lines, 2, STREAMS, stream, units), LOW),
        all_gpre=((lines, 2, STREAMS, stream, units), LOW),
        all_mix=((lines, 2, STREAMS, stream, head_width), LOW),
        all_dqkv=((lines, 2, 3, STREAMS, stream, head_width), LOW),
    )
    outputs = dict(**sums, **gathered)
    scratch = dict(
        wq=vmem((lines,) + weights["wq_in"].shape, LOW),
        wo=vmem((lines,) + weights["wo_in"].shape, LOW),
        wf=vmem((lines,) + weights["wf_in"].shape, LOW),
        wp=vmem((lines,) + weights["wp_in"].shape, LOW),
        small_own=vmem((8, width), F32),
        small=vmem((lines, 8, width), F32),
        count_own=vmem((lines, 8, total), F32),
        count=vmem((lines, 8, total), F32),
        hidden=vmem((STREAMS, owned, width), F32),
        middle=vmem((STREAMS, owned, width), F32),
        upstream=vmem((STREAMS, owned, width), LOW),
        first_out=vmem((2, owned, width), LOW),
        first_in=vmem((STREAMS, 2, owned, width), LOW),
        xhat1=vmem((lines, STREAMS, owned, width), F32),
        inv1=vmem((lines, STREAMS, owned, 128), F32),
        xhat2=vmem((lines, STREAMS, owned, width), F32),
        inv2=vmem((lines, STREAMS, owned, 128), F32),
        nrm=vmem((lines, STREAMS, stream, width), LOW),
        nmlp=vmem((lines, STREAMS, stream, width), LOW),
        ups=vmem((lines, STREAMS, stream, width), LOW),
        brn=vmem((lines, STREAMS, stream, width), LOW),
        act=vmem((lines, STREAMS, stream, units), LOW),
        gpre=vmem((lines, STREAMS, stream, units), LOW),
        slope=vmem((lines, STREAMS, stream, units), F32),
        mix=vmem((lines, STREAMS, stream, head_width), LOW),
        qry=vmem((lines, STREAMS, stream, head_width), LOW),
        gmix=vmem((STREAMS, stream, head_width), LOW),
        dqkv=vmem((lines, 3, STREAMS, stream, head_width), LOW),
        pass_ups=vmem((STREAMS, stream, width), LOW),
        pass_gpre=vmem((STREAMS, stream, units), LOW),
        kv=vmem((lines, 2, total, head_width), LOW),
        soft=vmem((lines, STREAMS, heads, stream, total), F32),
        near=vmem((STREAMS, stream, total), F32),
        dkv_all=vmem((2, total, head_width), F32),
        dkv_out=vmem((lines, 2, local, head_width), LOW),
        dkv_in=vmem((lines, 2, local, head_width), LOW),
        part=vmem((4, STREAMS, stream, width), LOW),
        arrived=vmem((lines, 4, STREAMS, peers, owned, width), LOW),
        out_low=vmem((lines, STREAMS, owned, width), LOW),
        grad_low=vmem((lines, STREAMS, owned, width), LOW),
        norm_part=vmem((lines, 8, width), F32),
        norm_all=vmem((lines, 8, width), F32),
        w_first_s=dma((4, 2)),
        w_first_r=dma((lines, 4)),
        w_second_s=dma((lines, 4)),
        w_second_r=dma((lines, 4, 2)),
        w_core_s=dma((lines, 4)),
        w_core_r=dma((lines, 4)),
        w_own=dma((4,)),
        small_s=dma((lines - 1,)),
        small_r=dma((lines,)),
        count_s=dma((lines - 1,)),
        count_r=dma((lines,)),
        ag_s=dma((4, STREAMS, peers)),
        ag_r=dma((4, STREAMS, peers)),
        rs_s=dma((4, STREAMS, peers)),
        rs_r=dma((4, STREAMS, peers)),
        kv_s=dma((lines, STREAMS)),
        kv_r=dma((lines, STREAMS)),
        dkv_s=dma((lines,)),
        dkv_r=dma((lines,)),
        rows_s=dma((8, lines, 2)),
        rows_r=dma((8,)),
        pass_s=dma((2,)),
        pass_r=dma((2,)),
        pass_on_s=dma((2, 2)),
        share_s=dma((4,)),
        share_r=dma((4,)),
        heads_r=dma((lines,)),
        heads_s=dma((lines,)),
        heads_sr=dma((lines,)),
        first_s=dma,
        first_r=dma((STREAMS,)),
        out_s=dma((lines, STREAMS)),
        out_r=dma,
        grad_s=dma((lines, STREAMS)),
        grad_r=dma,
        norm_s=dma((lines,)),
        norm_r=dma,
        ends_s=dma((2 * chips - 1,)),
        ends_r=dma,
    )
    names = tuple(operands) + tuple(outputs) + tuple(scratch)
    results = pl.pallas_call(
        functools.partial(relay_kernel, names),
        out_shape=[jax.ShapeDtypeStruct(shape, kind) for shape, kind in outputs.values()],
        in_specs=[pl.BlockSpec(memory_space=space(name)) for name in operands],
        out_specs=[
            pl.BlockSpec(memory_space=pl.ANY if name in gathered else pltpu.VMEM)
            for name in outputs
        ],
        scratch_shapes=list(scratch.values()),
        compiler_params=pltpu.CompilerParams(
            collective_id=0, has_side_effects=True, vmem_limit_bytes=60 * 2**20
        ),
        name="relay",
    )(*operands.values())
    return dict(zip(outputs, results))


def weights_kernel(names, *refs):
    r = types.SimpleNamespace(**dict(zip(names, refs)))
    micro_count, rows, buckets, width = r.activations.shape
    chips, units, head_width = r.ends.shape[0] // 2, r.all_act.shape[-1], r.all_mix.shape[-1]
    lines = r.acts.shape[0]
    loads = [
        pltpu.make_async_copy(source, target, r.load_sem.at[place])
        for place, (source, target) in enumerate(
            (
                (r.all_act, r.act),
                (r.all_ups, r.ups),
                (r.all_nmlp, r.nmlp),
                (r.all_gpre, r.gpre),
                (r.all_mix, r.mix),
                (r.all_brn, r.brn),
                (r.all_nrm, r.nrm),
                (r.all_dqkv, r.dqkv),
            )
        )
    ]
    stores = [
        pltpu.make_async_copy(source, target, r.store_sem.at[place])
        for place, (source, target) in enumerate(
            (
                (r.own_proj, r.w_proj),
                (r.own_fc, r.w_fc),
                (r.own_out, r.w_out),
                (r.own_qkv, r.w_qkv),
            )
        )
    ]
    for load in loads:
        load.start()

    sums = r.ends[0]
    for other in range(1, 2 * chips):
        sums = sums + r.ends[other]
    singles = (r.ln1_gain, r.ln1_shift, r.ln2_gain, r.ln2_shift, r.b_out, r.b_proj)
    for place, single in enumerate(singles):
        single[...] = sums[place : place + 1]
    for chip in range(chips):
        both = r.ends[chip] + r.ends[chips + chip]
        r.b_fc[:, chip * units : (chip + 1) * units] = both[6:7, :units]
        here = slice(chip * head_width, (chip + 1) * head_width)
        r.b_qv[0:1, here] = both[7:8, :head_width]
        r.b_qv[1:2, here] = both[7:8, width // 2 : width // 2 + head_width]
    for target, source in ((r.activations, r.acts), (r.in_grads, r.grads)):
        for micro in range(micro_count):
            rows_of = [
                source[micro * buckets + bucket].astype(F32)[:, None, :]
                for bucket in range(buckets)
            ]
            target[micro] = jnp.concatenate(rows_of, axis=1).astype(LOW)

    def flat(array):
        return array.reshape(lines * 2 * chips * rows, array.shape[-1])

    loads[0].wait()
    loads[1].wait()
    r.own_proj[...] = dot_tn(flat(r.act[...]), flat(r.ups[...]))
    stores[0].start()
    loads[2].wait()
    loads[3].wait()
    r.own_fc[...] = dot_tn(flat(r.nmlp[...]), flat(r.gpre[...]))
    stores[1].start()
    loads[4].wait()
    loads[5].wait()
    r.own_out[...] = dot_tn(flat(r.mix[...]), flat(r.brn[...]))
    stores[2].start()
    loads[6].wait()
    loads[7].wait()
    nrm = flat(r.nrm[...])
    for which in range(3):
        r.own_qkv[which] = dot_tn(flat(r.dqkv[:, :, which]), nrm)
    stores[3].start()
    for store in stores:
        store.wait()


def weights_call(relayed, inputs_shape, head_width, units):
    chips = lax.axis_size("tensor")
    width = inputs_shape[-1]
    half = width // 2
    outputs = dict(
        activations=(inputs_shape, LOW),
        in_grads=(inputs_shape, LOW),
        ln1_gain=((1, width), F32),
        ln1_shift=((1, width), F32),
        w_qkv=((3, head_width, half), F32),
        b_qv=((2, width), F32),
        w_out=((head_width, half), F32),
        b_out=((1, width), F32),
        ln2_gain=((1, width), F32),
        ln2_shift=((1, width), F32),
        w_fc=((half, units), F32),
        b_fc=((1, chips * units), F32),
        w_proj=((units, half), F32),
        b_proj=((1, width), F32),
    )
    rows = ("act", "ups", "nmlp", "gpre", "mix", "brn", "nrm", "dqkv")
    own = dict(own_proj="w_proj", own_fc="w_fc", own_out="w_out", own_qkv="w_qkv")
    scratch = {name: pltpu.VMEM(relayed["all_" + name].shape, LOW) for name in rows}
    scratch.update({name: pltpu.VMEM(outputs[of][0], F32) for name, of in own.items()})
    scratch["load_sem"] = pltpu.SemaphoreType.DMA((8,))
    scratch["store_sem"] = pltpu.SemaphoreType.DMA((4,))
    whole, apart = pl.BlockSpec(memory_space=pltpu.VMEM), pl.BlockSpec(memory_space=pl.ANY)
    small = ("acts", "grads", "ends")
    return pl.pallas_call(
        functools.partial(weights_kernel, tuple(relayed) + tuple(outputs) + tuple(scratch)),
        out_shape=[jax.ShapeDtypeStruct(shape, kind) for shape, kind in outputs.values()],
        in_specs=[whole if name in small else apart for name in relayed],
        out_specs=[apart if name in own.values() else whole for name in outputs],
        scratch_shapes=list(scratch.values()),
        compiler_params=pltpu.CompilerParams(vmem_limit_bytes=60 * 2**20),
        name="weight_gradients",
    )(*relayed.values())


def on_line(
    inputs,
    cotangent,
    lengths,
    chosen,
    ln1_gain,
    ln1_shift,
    w_qkv,
    b_qv,
    w_out,
    b_out,
    ln2_gain,
    ln2_shift,
    w_fc,
    b_fc,
    w_proj,
    b_proj,
):
    head_width, units = w_out.shape[1], w_fc.shape[2]
    singles = dict(
        ln1_gain=ln1_gain,
        ln1_shift=ln1_shift,
        ln2_gain=ln2_gain,
        ln2_shift=ln2_shift,
        b_out=b_out,
        b_proj=b_proj,
        b_fc=b_fc,
        b_qv=b_qv[0],
    )
    weights = dict(
        wq_in=jnp.swapaxes(w_qkv[0], 1, 2).reshape(-1, inputs.shape[-1]),
        wo_in=w_out[0],
        wf_in=w_fc[0],
        wp_in=w_proj[0],
    )
    picks = chosen.reshape((-1,) + chosen.shape[-2:])
    relayed = relay_call(inputs, cotangent, lengths, picks, singles, weights)
    results = list(weights_call(relayed, inputs.shape, head_width, units))
    results[4] = jnp.swapaxes(results[4], 1, 2)
    vectors = (2, 3, 7, 8, 9, 11, 13)
    return tuple(
        result if place in vectors else result[None] for place, result in enumerate(results)
    )


def fits_lines(mesh):
    return mesh.shape["section"] == 4 and mesh.shape["seq"] == 2 and mesh.shape["tensor"] == 4


def solution(mesh):
    placed = (
        P(None, ("seq", "tensor"), None, None),
        P(None, ("seq", "tensor"), None, None),
        P(),
        P("section", None, None, "tensor", "seq", None),
        P("section", None),
        P("section", None),
        P("section", None, None, "tensor"),
        P("section", None, "tensor"),
        P("section", "tensor", None),
        P("section", None),
        P("section", None),
        P("section", None),
        P("section", None, "tensor"),
        P("section", "tensor"),
        P("section", "tensor", None),
        P("section", None),
    )
    return jax.shard_map(
        on_line if fits_lines(mesh) else on_device,
        mesh=mesh,
        in_specs=placed,
        out_specs=(
            P("section", None, ("seq", "tensor"), None, None),
            P("section", None, ("seq", "tensor"), None, None),
            P("section", None),
            P("section", None),
            P("section", None, "seq", "tensor"),
            P("section", None, None),
            P("section", "tensor", "seq"),
            P("section", None),
            P("section", None),
            P("section", None),
            P("section", "seq", "tensor"),
            P("section", None),
            P("section", "tensor", "seq"),
            P("section", None),
        ),
        check_vma=False,
    )
```
